32 devices in a mesh: batch: 4 (over z), tile: 8 (over y, x, core).
Axes of the slice: x: 2, y: 2, z: 4, core: 2. Of those that a mesh axis runs over, the one named last changes fastest.
Arguments:
- pixels: bfloat16 [4, 8, 8, 9, 36, 128], P('batch', 'tile'), may hold values from -6 to 6
- buckets: int32 [64], P('batch'), may hold values from 0 to 2
- slot_owner_table: int32 [328], replicated, may hold values from 0 to 327, each once
- out_grad: bfloat16 [4, 8, 2, 1, 18, 18, 320], P('batch', 'tile'), may hold values from -6 to 6
- master: float32 [328, 64, 64], P('tile'), may hold values from -0.25 to 0.25
- left_stat: float32 [328, 64, 64], P('tile'), as said below
- right_stat: float32 [328, 64, 64], P('tile'), as said below
- left_root: float32 [328, 64, 64], P('tile'), as said below
- right_root: float32 [328, 64, 64], P('tile'), as said below
- vectors: float32 [5248], replicated, may hold values from 0.5 to 1.5
- moment: float32 [5248], P('tile'), as said below
Outputs:
- result: float32 [4, 8, 2, 1, 18, 18, 320], P('batch', 'tile')
- pixel_grad: float32 [4, 8, 8, 9, 36, 128], P('batch', 'tile')
- clip_norm: float32 [], replicated
- block_grad: float32 [328, 64, 64], P('tile')
- left_new: float32 [328, 64, 64], P('tile')
- right_new: float32 [328, 64, 64], P('tile')
- master_new: float32 [328, 64, 64], P('tile')
- weight_copy: bfloat16 [328, 64, 64], P('tile')
- vec_grad: float32 [5248], P('tile')
- vec_moment: float32 [5248], P('tile')
- vec_new: float32 [5248], P('tile')
The draws below stay inside these ranges and needn't reach their ends.
Inputs may be any that keep to these rules, and one draw needn't show every extreme that they name: `slot_owner_table`: slot s of the tile device p is entry p * 41 + s. `left_stat`: symmetric blocks with a positive diagonal. `right_stat`: symmetric blocks with a positive diagonal. `left_root`: symmetric blocks with a positive diagonal. `right_root`: symmetric blocks with a positive diagonal. `moment`: positive.
All inputs are finite; a program needn't handle non-finite values.
Results may differ from the reference program's by a relative error of at most 0.011.
Values may be sent and summed in bfloat16 or wider, within the bound.
No kernel may reach another device: no remote copies, remote signals or barrier semaphores. Data moves between devices by JAX's collectives and lax.ppermute only.
A program may use at most 576 MiB of HBM per device.

```python
import jax
import jax.numpy as jnp
from jax import lax

C2 = 128
HID2 = 512
C3 = 320
HID3 = 1280
CH = 36
CW = 36
STRIPS = 4
IPP = 1
BS = 64
SR = 9
H3 = 18
W3 = 18
GROUPS = 2
SLOTS = 8
IMAGES = 64
NBR = 322
BLOCK_SLOTS_ALL = 328
VEC = 5248
N_BATCH = 4
N_TILE = 8


def stat_blocks(key, diagonal_scale):
    first_key, second_key = jax.random.split(key)
    spread_draw = jax.random.uniform(first_key, (BLOCK_SLOTS_ALL, BS), jnp.float32)
    diagonal = diagonal_scale * jnp.exp(jnp.log(4.0) * spread_draw)
    off_part = jax.random.normal(second_key, (BLOCK_SLOTS_ALL, BS, BS), jnp.float32) * (diagonal_scale / BS)
    off_part = 0.5 * (off_part + jnp.swapaxes(off_part, 1, 2))
    positions = jnp.arange(BS)
    on_diagonal = positions[:, None] == positions[None, :]
    return jnp.where(on_diagonal[None], diagonal[:, :, None], off_part)


def draw_left_stat(key, part):
    key = jax.random.fold_in(key, 11)
    return stat_blocks(key, 1.0 / (NBR * BS))


def draw_right_stat(key, part):
    key = jax.random.fold_in(key, 12)
    return stat_blocks(key, 1.0 / (NBR * BS))


def draw_left_root(key, part):
    key = jax.random.fold_in(key, 13)
    return stat_blocks(key, 0.5 * (NBR * BS) ** 0.25)


def draw_right_root(key, part):
    key = jax.random.fold_in(key, 14)
    return stat_blocks(key, 0.5 * (NBR * BS) ** 0.25)


def draw_moment(key, part):
    key = jax.random.fold_in(key, 15)
    spread_draw = jax.random.uniform(key, (VEC,), jnp.float32)
    return jnp.exp(jnp.log(4.0) * spread_draw) / (NBR * BS * BS + VEC)


def plant(values, stream_key, low, largest):
    extent = values.shape
    spot = [jax.random.randint(jax.random.fold_in(stream_key, axis), (), 0, extent[axis]) for axis in range(len(extent))]
    values = values.at[tuple(spot)].set(low)
    longest = extent.index(max(extent))
    spot[longest] = (spot[longest] + 1) % extent[longest]
    return values.at[tuple(spot)].set(largest)


def steps_of(rng, dims, cuts, least, high):
    loudness, own = 1.0, jax.random.fold_in(rng, 6)
    for dim, shards_of in cuts:
        draws = jnp.exp(jax.random.uniform(jax.random.fold_in(own, dim), (shards_of,), jnp.float32, least / len(cuts), high / len(cuts)))
        loudness = loudness * jnp.repeat(draws, dims[dim] // shards_of).reshape([-1 if axis == dim else 1 for axis in range(len(dims))])
    return loudness


def bell_draw(own_key, extent, width, limit, cuts=(), held_as=jnp.bfloat16):
    values = width * jax.random.normal(own_key, extent, jnp.float32)
    if cuts:
        values = values * steps_of(own_key, extent, cuts, -0.22, 0.18)
    return jnp.clip(values, -limit, limit).astype(held_as)


def setup_inputs(seed: int = 0) -> dict:
    key_list = jax.random.split(jax.random.key(seed), 12)
    pixels = bell_draw(key_list[0], (N_BATCH, N_TILE, SLOTS, SR, CW, C2), 1.0, 6.0, ((0, 4), (1, 8)))
    buckets = plant(jax.random.randint(key_list[1], (IMAGES,), 0, 3), jax.random.fold_in(key_list[1], 1), 0, 2).astype(jnp.int32)
    slot_owner_table = jax.random.permutation(key_list[2], BLOCK_SLOTS_ALL).astype(jnp.int32)
    out_grad = bell_draw(key_list[3], (N_BATCH, N_TILE, GROUPS, IPP, H3, W3, C3), 1.0, 6.0, ((0, 4), (1, 8)))
    master = bell_draw(key_list[4], (BLOCK_SLOTS_ALL, BS, BS), HID2 ** -0.5, 0.25, ((0, 8),), jnp.float32)
    left_stat = draw_left_stat(jax.random.fold_in(key_list[11], 71), 0)
    right_stat = draw_right_stat(jax.random.fold_in(key_list[11], 71), 0)
    left_root = draw_left_root(jax.random.fold_in(key_list[11], 71), 0)
    right_root = draw_right_root(jax.random.fold_in(key_list[11], 71), 0)
    vectors = jnp.clip(jax.random.uniform(key_list[9], (VEC,), jnp.float32, 0.5, 1.5), 0.5, 1.5)
    moment = draw_moment(jax.random.fold_in(key_list[11], 71), 0)
    return {"pixels": pixels, "buckets": buckets, "slot_owner_table": slot_owner_table, "out_grad": out_grad, "master": master, "left_stat": left_stat, "right_stat": right_stat, "left_root": left_root, "right_root": right_root, "vectors": vectors, "moment": moment}


eps_norm = 1e-05
clip_limit = 1.0
rate_matrix = 0.3
rate_vector = 0.3
eps_adagrad = 1e-08
images_each = 4
highest = lax.Precision.HIGHEST

@jax.custom_vjp
def low(v):
    return lax.optimization_barrier(v.astype(jnp.bfloat16)).astype(jnp.float32)

@jax.custom_vjp
def low_back(v):
    return v

def low_keep(v):
    return (low(v), None)

def low_pass(kept, grad):
    return (grad,)

def back_keep(v):
    return (v, None)

def back_low(kept, grad):
    return (low(grad),)
low.defvjp(low_keep, low_pass)
low_back.defvjp(back_keep, back_low)

def matrix_shapes():
    return [(C2, HID2), (HID2, C2), (9 * C2, C3), (C3, HID3), (HID3, C3)]

def unblock(blocks):
    matrix_list = []
    offset = 0
    for row_total, col_total in matrix_shapes():
        row_blocks, col_blocks = (row_total // BS, col_total // BS)
        stacked = blocks[offset:offset + row_blocks * col_blocks].reshape(row_blocks, col_blocks, BS, BS)
        matrix_list.append(stacked.transpose(0, 2, 1, 3).reshape(row_total, col_total))
        offset += row_blocks * col_blocks
    return tuple(matrix_list)

def resplit_blocks(matrix_list, overall_block_count):
    stacks = []
    for matrix in matrix_list:
        row_total, col_total = matrix.shape
        stacks.append(matrix.reshape(row_total // BS, BS, col_total // BS, BS).transpose(0, 2, 1, 3).reshape(-1, BS, BS))
    joined = jnp.concatenate(stacks, axis=0)
    filler = jnp.zeros((overall_block_count - joined.shape[0], BS, BS), joined.dtype)
    return jnp.concatenate([joined, filler], axis=0)

def split_vector(values):
    lengths = [C2] * 6 + [HID2, C2, C3] + [C3] * 6 + [HID3, C3]
    pieces = []
    offset = 0
    for length in lengths:
        pieces.append(values[offset:offset + length])
        offset += length
    return (tuple(pieces[:8]), pieces[8], tuple(pieces[9:]))

def canvas_mask(bucket_ids, row_index, col_index):
    heights = jnp.where(bucket_ids == 0, 5 * CH // 9, jnp.where(bucket_ids == 1, 7 * CH // 9, CH))
    breadths = jnp.where(bucket_ids == 0, CW, jnp.where(bucket_ids == 1, 7 * CW // 9, 5 * CW // 9))
    rows_inside = (row_index[None, :] >= 0) & (row_index[None, :] < heights[:, None])
    cols_inside = col_index[None, :] < breadths[:, None]
    return (rows_inside[:, :, None] & cols_inside[:, None, :]).astype(jnp.float32)

def multiply(left, right):
    return jnp.einsum('...c,cd->...d', left, right, precision=highest)

def group_norm(values, valid, gain, bias):
    weight = valid[..., None]
    counts = lax.optimization_barrier(jnp.sum(valid, axis=(1, 2))) * values.shape[-1]
    mean_value = lax.optimization_barrier(jnp.sum(values * weight, axis=(1, 2, 3))) / counts
    mean_square = lax.optimization_barrier(jnp.sum(values * values * weight, axis=(1, 2, 3))) / counts
    scaling = lax.rsqrt(mean_square - mean_value * mean_value + eps_norm)
    return (values - mean_value[:, None, None, None]) * scaling[:, None, None, None] * gain + bias

def window_sum(values):
    padded = jnp.pad(values, [(0, 0), (1, 1), (1, 1)] + [(0, 0)] * (values.ndim - 3))
    row_count, col_count = (values.shape[1], values.shape[2])
    running_totals = jnp.zeros_like(values)
    for row_step in range(3):
        for col_step in range(3):
            running_totals = running_totals + padded[:, row_step:row_step + row_count, col_step:col_step + col_count]
    return running_totals

def meta_block(values, valid, params, weight_in, weight_out):
    gain_one, bias_one, scale_one, gain_two, bias_two, scale_two, hidden_bias, out_bias = params
    weight = valid[..., None]
    normed = low(group_norm(values, valid, gain_one, bias_one))
    pooled = window_sum(normed * weight) / jnp.maximum(window_sum(valid), 1.0)[..., None] - normed
    mixed = values + scale_one * weight * pooled
    normed_two = low(group_norm(mixed, valid, gain_two, bias_two))
    hidden = low_back(multiply(normed_two, weight_in) + hidden_bias)
    active = low(jax.nn.gelu(hidden, approximate=False))
    branch = low_back(multiply(active, weight_out) + out_bias)
    return mixed + scale_two * weight * branch

def embed(zed, valid, weight, bias):
    padded = jnp.pad(zed, ((0, 0), (1, 1), (1, 1), (0, 0)))
    row_count, col_count = (zed.shape[1], zed.shape[2])
    patches = jnp.concatenate([padded[:, row_step:row_step + row_count:2, col_step:col_step + col_count:2] for row_step in range(3) for col_step in range(3)], axis=-1)
    return valid[..., None] * low_back(multiply(patches, weight) + bias)

def network(values, matrix_list, vector_values, first_mask, second_mask):
    first_params, embed_bias, second_params = split_vector(vector_values)
    first_out = meta_block(values, first_mask, first_params, matrix_list[0], matrix_list[1])
    zed = low_back(low(first_out * first_mask[..., None]))
    embedded = embed(zed, second_mask, matrix_list[2], embed_bias)
    return meta_block(embedded, second_mask, second_params, matrix_list[3], matrix_list[4])

def reference(pixels, buckets, slot_owner_table, out_grad, master, left_stat, right_stat, left_root, right_root, vectors, moment):
    steps_total = IMAGES // images_each
    images = jnp.roll(pixels.astype(jnp.float32), 2, axis=1).reshape(N_BATCH, GROUPS, STRIPS, SLOTS, SR, CW, C2)
    images = images.transpose(0, 1, 3, 2, 4, 5, 6).reshape(steps_total, images_each, CH, CW, C2)
    targets = out_grad.astype(jnp.float32).transpose(0, 2, 1, 3, 4, 5, 6).reshape(steps_total, images_each, H3, W3, C3)
    bucket_rows = buckets.reshape(steps_total, images_each)
    by_number = jnp.zeros((BLOCK_SLOTS_ALL, BS, BS), jnp.float32).at[slot_owner_table].set(low(master))
    matrix_list = unblock(by_number)

    def one_step(carry, inputs):
        values, cotangent, bucket_ids = inputs
        first_mask = canvas_mask(bucket_ids, jnp.arange(CH, dtype=jnp.int32), jnp.arange(CW, dtype=jnp.int32))
        second_mask = canvas_mask(bucket_ids, 2 * jnp.arange(H3, dtype=jnp.int32), 2 * jnp.arange(W3, dtype=jnp.int32))
        output, backward = jax.vjp(lambda first, second, third: network(first, second, third, first_mask, second_mask), values, matrix_list, vectors)
        d_values, d_matrices, d_vector = backward(cotangent)
        carry = (tuple((old + new for old, new in zip(carry[0], d_matrices))), carry[1] + d_vector)
        return (carry, (output, d_values))
    start = (tuple((jnp.zeros_like(matrix) for matrix in matrix_list)), jnp.zeros_like(vectors))
    running_totals, (outputs, d_images) = lax.scan(one_step, start, (images, targets, bucket_rows))
    result = outputs.reshape(N_BATCH, GROUPS, N_TILE, IPP, H3, W3, C3).transpose(0, 2, 1, 3, 4, 5, 6)
    pixel_grad = d_images.reshape(N_BATCH, GROUPS, SLOTS, STRIPS, SR, CW, C2).transpose(0, 1, 3, 2, 4, 5, 6)
    pixel_grad = jnp.roll(pixel_grad.reshape(N_BATCH, N_TILE, SLOTS, SR, CW, C2), -2, axis=1)
    unsplit_block_list = resplit_blocks(list(running_totals[0]), BLOCK_SLOTS_ALL)[slot_owner_table]
    raw_vector = running_totals[1]
    clip_norm = jnp.sqrt(jnp.sum(unsplit_block_list * unsplit_block_list) + jnp.sum(raw_vector * raw_vector))
    factor = jnp.minimum(1.0, clip_limit / clip_norm)
    block_grad = unsplit_block_list * factor
    left_new = 0.5 * left_stat + 0.5 * jnp.einsum('sij,skj->sik', block_grad, block_grad, precision=highest)
    right_new = 0.5 * right_stat + 0.5 * jnp.einsum('sji,sjk->sik', block_grad, block_grad, precision=highest)
    stepped = jnp.einsum('sij,sjk->sik', left_root, block_grad, precision=highest)
    stepped = jnp.einsum('sij,sjk->sik', stepped, right_root, precision=highest)
    master_new = master - rate_matrix * stepped
    vec_grad = raw_vector * factor
    vec_moment = moment + vec_grad * vec_grad
    vec_new = vectors - rate_vector * vec_grad / (jnp.sqrt(vec_moment) + eps_adagrad)
    return (result, pixel_grad, clip_norm, block_grad, left_new, right_new, master_new, master_new.astype(jnp.bfloat16), vec_grad, vec_moment, vec_new)
```

```python
import jax
import jax.numpy as jnp
from jax import lax
from jax.sharding import PartitionSpec as P

C2 = 128
HID2 = 512
C3 = 320
HID3 = 1280
CH = 36
CW = 36
STRIPS = 4
BS = 64


eps_norm = 1e-05
clip_limit = 1.0
rate_matrix = 0.3
rate_vector = 0.3
eps_adagrad = 1e-08
highest = lax.Precision.HIGHEST


def with_halo(cells, sides, width):
    for axis, dim in sides:
        count = lax.axis_size(axis)
        head = lax.slice_in_dim(cells, 0, width, axis=dim)
        tail = lax.slice_in_dim(cells, cells.shape[dim] - width, cells.shape[dim], axis=dim)
        cells = jnp.concatenate(
            [
                lax.ppermute(tail, axis, [(i, (i + 1) % count) for i in range(count)]),
                cells,
                lax.ppermute(head, axis, [((i + 1) % count, i) for i in range(count)]),
            ],
            axis=dim,
        )
    return cells


def matrix_shapes():
    return [(C2, HID2), (HID2, C2), (9 * C2, C3), (C3, HID3), (HID3, C3)]


def unblock(blocks):
    matrix_list = []
    offset = 0
    for row_total, col_total in matrix_shapes():
        row_blocks, col_blocks = (row_total // BS, col_total // BS)
        stacked = blocks[offset : offset + row_blocks * col_blocks].reshape(
            row_blocks, col_blocks, BS, BS
        )
        matrix_list.append(stacked.transpose(0, 2, 1, 3).reshape(row_total, col_total))
        offset += row_blocks * col_blocks
    return tuple(matrix_list)


def resplit_blocks(matrix_list, overall_block_count):
    stacks = []
    for matrix in matrix_list:
        row_total, col_total = matrix.shape
        stacks.append(
            matrix.reshape(row_total // BS, BS, col_total // BS, BS)
            .transpose(0, 2, 1, 3)
            .reshape(-1, BS, BS)
        )
    joined = jnp.concatenate(stacks, axis=0)
    filler = jnp.zeros((overall_block_count - joined.shape[0], BS, BS), joined.dtype)
    return jnp.concatenate([joined, filler], axis=0)


def split_vector(values):
    lengths = [C2] * 6 + [HID2, C2, C3] + [C3] * 6 + [HID3, C3]
    pieces = []
    offset = 0
    for length in lengths:
        pieces.append(values[offset : offset + length])
        offset += length
    return (tuple(pieces[:8]), pieces[8], tuple(pieces[9:]))


def canvas_mask(bucket_ids, row_index, col_index):
    heights = jnp.where(bucket_ids == 0, 5 * CH // 9, jnp.where(bucket_ids == 1, 7 * CH // 9, CH))
    breadths = jnp.where(bucket_ids == 0, CW, jnp.where(bucket_ids == 1, 7 * CW // 9, 5 * CW // 9))
    rows_inside = (row_index[None, :] >= 0) & (row_index[None, :] < heights[:, None])
    cols_inside = col_index[None, :] < breadths[:, None]
    return (rows_inside[:, :, None] & cols_inside[:, None, :]).astype(jnp.float32)


def multiply(left, right):
    flat = left.reshape(-1, left.shape[-1])
    return jnp.dot(flat, right, preferred_element_type=jnp.float32).reshape(
        left.shape[:-1] + (right.shape[1],)
    )


def contract(left, right):
    return lax.dot_general(
        left.reshape(-1, left.shape[-1]),
        right.reshape(-1, right.shape[-1]),
        (((0,), (0,)), ((), ())),
        preferred_element_type=jnp.float32,
    )


def window_cols(values):
    chans = values.shape[3] if values.ndim == 4 else 1
    count, rows, cols = (values.shape[0], values.shape[1], values.shape[2])
    flat = values.reshape(count, rows, cols * chans)
    zeros = jnp.zeros((count, rows, chans), flat.dtype)
    summed = flat + jnp.concatenate([zeros, flat[..., :-chans]], axis=-1)
    summed = summed + jnp.concatenate([flat[..., chans:], zeros], axis=-1)
    return summed.reshape(values.shape)


def window_rows(values):
    stacked = values[:, :-2] + values[:, 1:-1] + values[:, 2:]
    return window_cols(stacked)


def pad_rows(values):
    return jnp.pad(values, [(0, 0), (1, 1)] + [(0, 0)] * (values.ndim - 2))


def unchanged(values):
    return values


def rows_forward(values):
    return with_halo(values, (("tile", 1),), 1)


def rows_backward(values):
    return with_halo(values.astype(jnp.bfloat16), (("tile", 1),), 1).astype(values.dtype)


def group_total(pieces):
    strip_place = (lax.axis_index("tile") + 2) % STRIPS
    window = pieces[None]
    for round_index in range(3):
        padded = with_halo(window, (("tile", 0),), window.shape[0])
        window = jnp.concatenate([padded[:1], window, padded[-1:]], axis=0)
    offsets = jnp.arange(7, dtype=jnp.int32) - 3
    member = ((offsets >= -strip_place) & (offsets <= 3 - strip_place)).astype(jnp.float32)
    return jnp.sum(member.reshape((7,) + (1,) * pieces.ndim) * window, axis=0)


def gelu_exact(values):
    return jax.nn.gelu(values, approximate=False)


def norm_forward(values, valid, gain, bias, total):
    weight = valid[..., None]
    weighted = values * weight
    pieces = jnp.stack(
        [
            jnp.sum(valid, axis=(1, 2)) * values.shape[-1],
            jnp.sum(weighted, axis=(1, 2, 3)),
            jnp.sum(weighted * values, axis=(1, 2, 3)),
        ]
    )
    sums = total(pieces)
    mean_value = sums[1] / sums[0]
    scaling = lax.rsqrt(sums[2] / sums[0] - mean_value * mean_value + eps_norm)
    normal = (values - mean_value[:, None, None, None]) * scaling[:, None, None, None]
    return (normal * gain + bias, (normal, scaling, sums[0]))


def norm_backward(gradient, valid, gain, kept, total):
    normal, scaling, counts = kept
    weight = valid[..., None]
    shaped = gradient * gain
    pieces = jnp.stack(
        [
            jnp.sum(shaped * weight, axis=(1, 2, 3)),
            jnp.sum(shaped * normal * weight, axis=(1, 2, 3)),
        ]
    )
    means = total(pieces) / counts
    back = (
        weight
        * scaling[:, None, None, None]
        * (shaped - means[0][:, None, None, None] - normal * means[1][:, None, None, None])
    )
    return (back, jnp.sum(gradient * normal, axis=(0, 1, 2)), jnp.sum(gradient, axis=(0, 1, 2)))


def block_forward(values, mask_full, params, weight_in, weight_out, spread, total):
    gain_one, bias_one, scale_one, gain_two, bias_two, scale_two, hidden_bias, out_bias = params
    valid = mask_full[:, 1:-1]
    weight = valid[..., None]
    normed, kept_one = norm_forward(values, valid, gain_one, bias_one, total)
    low_normed = normed.astype(jnp.bfloat16)
    widened = spread(low_normed).astype(jnp.float32) * mask_full[..., None]
    counts = jnp.maximum(window_rows(mask_full), 1.0)[..., None]
    pooled = window_rows(widened) / counts - low_normed.astype(jnp.float32)
    mixed = values + scale_one * weight * pooled
    normed_two, kept_two = norm_forward(mixed, valid, gain_two, bias_two, total)
    low_two = normed_two.astype(jnp.bfloat16)
    hidden = multiply(low_two, weight_in) + hidden_bias
    active = gelu_exact(hidden).astype(jnp.bfloat16)
    branch = multiply(active, weight_out) + out_bias
    output = mixed + scale_two * weight * branch
    return (output, (kept_one, pooled, counts, kept_two, low_two, hidden, active, branch))


def block_backward(gradient, saved, mask_full, params, weight_in, weight_out, spread, total):
    gain_one, bias_one, scale_one, gain_two, bias_two, scale_two, hidden_bias, out_bias = params
    kept_one, pooled, counts, kept_two, low_two, hidden, active, branch = saved
    valid = mask_full[:, 1:-1]
    weight = valid[..., None]
    low_grad = (scale_two * weight * gradient).astype(jnp.bfloat16)
    d_scale_two = jnp.sum(weight * branch * gradient, axis=(0, 1, 2))
    d_out_bias = jnp.sum(low_grad.astype(jnp.float32), axis=(0, 1, 2))
    d_weight_out = contract(active, low_grad)
    d_active = multiply(low_grad, weight_out.T)
    d_hidden = jax.vjp(gelu_exact, hidden)[1](d_active)[0]
    low_hidden = d_hidden.astype(jnp.bfloat16)
    d_hidden_bias = jnp.sum(low_hidden.astype(jnp.float32), axis=(0, 1, 2))
    d_weight_in = contract(low_two, low_hidden)
    d_normed_two = multiply(low_hidden, weight_in.T)
    d_mixed, d_gain_two, d_bias_two = norm_backward(d_normed_two, valid, gain_two, kept_two, total)
    d_mixed = d_mixed + gradient
    d_pool = scale_one * weight * d_mixed
    d_scale_one = jnp.sum(weight * pooled * d_mixed, axis=(0, 1, 2))
    widened = spread(d_pool / counts) * mask_full[..., None]
    d_normed = weight * window_rows(widened) - d_pool
    d_values, d_gain_one, d_bias_one = norm_backward(d_normed, valid, gain_one, kept_one, total)
    vector_grad = jnp.concatenate(
        [
            d_gain_one,
            d_bias_one,
            d_scale_one,
            d_gain_two,
            d_bias_two,
            d_scale_two,
            d_hidden_bias,
            d_out_bias,
        ]
    )
    return (d_values + d_mixed, d_weight_in, d_weight_out, vector_grad)


def shift_right(values):
    return jnp.concatenate([jnp.zeros_like(values[:, :, :1]), values[:, :, :-1]], axis=2)


def shift_left(values):
    return jnp.concatenate([values[:, :, 1:], jnp.zeros_like(values[:, :, :1])], axis=2)


def embed_sources(zed):
    count, rows, cols, chans = zed.shape
    pairs = zed.reshape(count, rows // 2, 2, cols // 2, 2 * chans)
    even_rows = pairs[:, :, 0]
    odd_rows = pairs[:, :, 1]
    above = jnp.concatenate([jnp.zeros_like(odd_rows[:, :1]), odd_rows[:, :-1]], axis=1)
    return (above, even_rows, odd_rows)


def embed_forward(zed, valid, weight, bias):
    sources = embed_sources(zed)
    chans = zed.shape[-1]
    summed = jnp.zeros(sources[0].shape[:3] + (weight.shape[1],), jnp.float32)
    for kernel_row in range(3):
        source = sources[kernel_row]
        base = 3 * kernel_row * chans
        summed = summed + multiply(source, weight[base + chans : base + 3 * chans])
        summed = summed + shift_right(multiply(source[..., chans:], weight[base : base + chans]))
    return (valid[..., None] * (summed + bias), sources)


def embed_backward(gradient, valid, sources, weight):
    low_grad = (valid[..., None] * gradient).astype(jnp.bfloat16)
    d_bias = jnp.sum(low_grad.astype(jnp.float32), axis=(0, 1, 2))
    chans = sources[0].shape[-1] // 2
    weight_rows = []
    d_sources = []
    for kernel_row in range(3):
        source = sources[kernel_row]
        base = 3 * kernel_row * chans
        weight_rows.append(contract(source[:, :, :-1, chans:], low_grad[:, :, 1:]))
        weight_rows.append(contract(source, low_grad))
        d_centre = multiply(low_grad, weight[base + chans : base + 3 * chans].T)
        d_left = shift_left(multiply(low_grad, weight[base : base + chans].T))
        d_sources.append(d_centre + jnp.concatenate([jnp.zeros_like(d_left), d_left], axis=-1))
    d_weight = jnp.concatenate(weight_rows, axis=0)
    d_even = d_sources[1]
    d_odd = d_sources[2] + jnp.concatenate(
        [d_sources[0][:, 1:], jnp.zeros_like(d_sources[0][:, :1])], axis=1
    )
    count, half_rows, half_cols = (d_even.shape[0], d_even.shape[1], d_even.shape[2])
    d_zed = jnp.stack([d_even, d_odd], axis=2).reshape(count, 2 * half_rows, 2 * half_cols, chans)
    return (d_zed, d_weight, d_bias)


def share_out(pieces, axis):
    return lax.all_to_all(pieces, axis, split_axis=0, concat_axis=0, tiled=True)


def to_all(piece, axis):
    count = lax.axis_size(axis)
    return share_out(jnp.broadcast_to(piece[None], (count,) + piece.shape), axis)


def strips_to_images(strips, group_count, per_piece):
    shaped = jnp.roll(strips, 2, axis=0)
    shaped = shaped.reshape((group_count, STRIPS, per_piece) + strips.shape[2:])
    shaped = shaped.transpose(0, 2, 1, 3, 4, 5)
    return shaped.reshape((group_count * per_piece, STRIPS * strips.shape[2]) + strips.shape[3:])


def images_to_strips(images, group_count, per_piece, tile_count):
    strip_rows = images.shape[1] // STRIPS
    shaped = images.reshape((group_count, per_piece, STRIPS, strip_rows) + images.shape[2:])
    shaped = shaped.transpose(0, 2, 1, 3, 4, 5)
    shaped = shaped.reshape((tile_count, per_piece, strip_rows) + images.shape[2:])
    return jnp.roll(shaped, -2, axis=0)


def on_device(
    pixels,
    buckets,
    slot_owner_table,
    out_grad,
    master,
    left_stat,
    right_stat,
    left_root,
    right_root,
    vectors,
    moment,
):
    tile_count = lax.axis_size("tile")
    tile_place = lax.axis_index("tile")
    slot_count = pixels.shape[2]
    per_piece = slot_count // tile_count
    group_count = tile_count // STRIPS
    owned = master.shape[0]
    strips = share_out(
        pixels.reshape((tile_count, per_piece) + pixels.shape[3:]), "tile"
    )
    first_in = strips_to_images(strips, group_count, per_piece).astype(jnp.float32)
    dense = master.astype(jnp.bfloat16).reshape(owned, BS // 2, 2 * BS)
    gathered = lax.all_gather(dense, "tile", axis=0, tiled=True).reshape(-1, BS, BS)
    block_grand_count = gathered.shape[0]
    numbers = jnp.arange(block_grand_count, dtype=jnp.int32)
    inverse = jnp.zeros_like(slot_owner_table).at[slot_owner_table].set(numbers)
    first_in_w, first_out_w, embed_w, second_in_w, second_out_w = unblock(
        jnp.take(gathered, inverse, axis=0)
    )
    first_params, embed_bias, second_params = split_vector(vectors)
    table = buckets.reshape(group_count, slot_count)
    image_ids = lax.dynamic_slice_in_dim(table, tile_place * per_piece, per_piece, 1).reshape(-1)
    small_mask = canvas_mask(
        image_ids,
        2 * jnp.arange(-1, CH // 2 + 1, dtype=jnp.int32),
        2 * jnp.arange(CW // 2, dtype=jnp.int32),
    )
    first_mask = canvas_mask(
        image_ids, jnp.arange(-1, CH + 1, dtype=jnp.int32), jnp.arange(CW, dtype=jnp.int32)
    )
    first_out, first_kept = block_forward(
        first_in, first_mask, first_params, first_in_w, first_out_w, pad_rows, unchanged
    )
    zed = (first_out * first_mask[:, 1:-1, :, None]).astype(jnp.bfloat16)
    embedded, sources = embed_forward(zed, small_mask[:, 1:-1], embed_w, embed_bias)
    result, second_kept = block_forward(
        embedded, small_mask, second_params, second_in_w, second_out_w, pad_rows, unchanged
    )
    incoming = out_grad[0, 0].astype(jnp.float32).reshape(result.shape)
    d_embedded, grad_second_input_weight, grad_second_output_weight, d_second_vec = block_backward(
        incoming,
        second_kept,
        small_mask,
        second_params,
        second_in_w,
        second_out_w,
        pad_rows,
        unchanged,
    )
    d_zed, grad_embedding_layer, d_embed_bias = embed_backward(
        d_embedded, small_mask[:, 1:-1], sources, embed_w
    )
    d_first = (
        d_zed.astype(jnp.bfloat16).astype(jnp.float32) * first_mask[:, 1:-1, :, None]
    )
    d_pixels, grad_first_input_weight, grad_first_output_weight, d_first_vec = block_backward(
        d_first,
        first_kept,
        first_mask,
        first_params,
        first_in_w,
        first_out_w,
        pad_rows,
        unchanged,
    )
    enumerated_items = resplit_blocks(
        [
            grad_first_input_weight,
            grad_first_output_weight,
            grad_embedding_layer,
            grad_second_input_weight,
            grad_second_output_weight,
        ],
        block_grand_count,
    )
    in_slots = jnp.take(enumerated_items.astype(jnp.bfloat16), slot_owner_table, axis=0)
    raw_vector = jnp.concatenate([d_first_vec, d_embed_bias, d_second_vec])
    share = raw_vector.shape[0] // tile_count
    vector_rows = -(-share // 128)
    vector_part = jnp.pad(
        raw_vector.reshape(tile_count, share), ((0, 0), (0, vector_rows * 128 - share))
    ).reshape(tile_count, vector_rows, 128)
    outgoing = jnp.concatenate(
        [
            in_slots.reshape(tile_count, owned * BS // 2, 2 * BS),
            vector_part.astype(jnp.bfloat16),
        ],
        axis=1,
    )
    tile_sum = jnp.sum(share_out(outgoing, "tile").astype(jnp.float32), axis=0)
    summed = jnp.sum(
        to_all(tile_sum.astype(jnp.bfloat16), "batch").astype(jnp.float32), axis=0
    )
    mine = summed[: owned * BS // 2].reshape(owned, BS, BS)
    mine_vector = summed[owned * BS // 2 :].reshape(-1)[:share]
    part = jnp.sum(summed * summed)
    square = jnp.sum(to_all(jnp.full((1, 128), part), "tile")[:, 0, 0])
    clip_norm = jnp.sqrt(square)
    factor = jnp.minimum(1.0, clip_limit / clip_norm)
    block_grad = mine * factor
    left_new = 0.5 * left_stat + 0.5 * jnp.einsum(
        "sij,skj->sik", block_grad, block_grad, precision=highest
    )
    right_new = 0.5 * right_stat + 0.5 * jnp.einsum(
        "sji,sjk->sik", block_grad, block_grad, precision=highest
    )
    stepped = jnp.einsum("sij,sjk->sik", left_root, block_grad, precision=highest)
    stepped = jnp.einsum("sij,sjk->sik", stepped, right_root, precision=highest)
    master_new = master - rate_matrix * stepped
    vec_grad = mine_vector * factor
    vec_moment = moment + vec_grad * vec_grad
    own_vectors = lax.dynamic_slice_in_dim(vectors, tile_place * share, share, 0)
    vec_new = own_vectors - rate_vector * vec_grad / (jnp.sqrt(vec_moment) + eps_adagrad)
    returned = share_out(
        images_to_strips(d_pixels.astype(jnp.bfloat16), group_count, per_piece, tile_count),
        "tile",
    )
    return (
        result.reshape(out_grad.shape),
        returned.astype(jnp.float32).reshape(pixels.shape),
        clip_norm,
        block_grad,
        left_new,
        right_new,
        master_new,
        master_new.astype(jnp.bfloat16),
        vec_grad,
        vec_moment,
        vec_new,
    )


def solution(mesh):
    placed = (
        P("batch", "tile", None, None, None, None),
        P("batch"),
        P(),
        P("batch", "tile", None, None, None, None, None),
        P("tile", None, None),
        P("tile", None, None),
        P("tile", None, None),
        P("tile", None, None),
        P("tile", None, None),
        P(),
        P("tile"),
    )
    return jax.shard_map(
        on_device,
        mesh=mesh,
        in_specs=placed,
        out_specs=(
            P("batch", "tile", None, None, None, None, None),
            P("batch", "tile", None, None, None, None),
            P(),
            P("tile", None, None),
            P("tile", None, None),
            P("tile", None, None),
            P("tile", None, None),
            P("tile", None, None),
            P("tile"),
            P("tile"),
            P("tile"),
        ),
        check_vma=False,
    )
```

```python
import functools

import jax
import jax.numpy as jnp
from jax import lax
from jax.experimental import pallas as pl
from jax.experimental.pallas import tpu as pltpu
from jax.sharding import PartitionSpec as P

C2 = 128
HID2 = 512
C3 = 320
HID3 = 1280
CH = 36
CW = 36
STRIPS = 4
BS = 64
SR = CH // STRIPS
H3 = CH // 2
W3 = CW // 2
WIDE = 384
LINE = 40
PLANE = H3 * LINE
ROWS = 6
CHUNK = ROWS * LINE
STEPS = H3 // ROWS
HALF = BS // 2

eps_norm = 1e-05
clip_limit = 1.0
rate_matrix = 0.3
rate_vector = 0.3
eps_adagrad = 1e-08
f32 = jnp.float32
bf16 = jnp.bfloat16

SHAPES = [(C2, HID2), (HID2, C2), (9 * C2, C3), (C3, HID3), (HID3, C3)]
USED = sum(rows // BS * (cols // BS) for rows, cols in SHAPES)
VEC_ROWS = (6 * C2 + HID2 + C2 + C3 + 6 * C3 + HID3 + C3) // 128
EXTRA = -(-VEC_ROWS // HALF)


def product(left, right):
    return jnp.dot(left, right, preferred_element_type=f32)


def product_nt(left, right):
    return lax.dot_general(left, right, (((1,), (1,)), ((), ())), preferred_element_type=f32)


def product_tn(left, right):
    return lax.dot_general(left, right, (((0,), (0,)), ((), ())), preferred_element_type=f32)


def gelu_pair(values):
    bell = jnp.exp2(values * values * (-0.5 * 1.4426950408889634))
    step = pl.reciprocal(1.0 + (0.3275911 * 0.7071067811865476) * jnp.abs(values), approx=True)
    tail = step * (
        0.5 * 0.254829592
        + step
        * (
            0.5 * -0.284496736
            + step
            * (0.5 * 1.421413741 + step * (0.5 * -1.453152027 + step * (0.5 * 1.061405429)))
        )
    )
    tail = tail * bell
    share = jnp.where(values >= 0.0, 1.0 - tail, tail)
    return (values * share, share + values * (bell * 0.3989422804014327))


def fold(values):
    chans = values.shape[-1]
    return jnp.sum(values.reshape(-1, 8, chans), axis=0)


def by_image(total):
    total = total + pltpu.roll(total, 4, 0)
    total = total + pltpu.roll(total, 2, 0)
    return jnp.sum(total, axis=1, keepdims=True)


def line(pattern):
    return jnp.concatenate([pattern] * (LINE // 8), axis=0)


def spread(pattern, chans):
    return line(jnp.broadcast_to(pattern, (8, chans)))


def from_left(values):
    flat = values.reshape(-1, values.shape[-1])
    return pltpu.roll(flat, 2, 0).reshape(values.shape)


def from_right(values):
    flat = values.reshape(-1, values.shape[-1])
    return pltpu.roll(flat, flat.shape[0] - 2, 0).reshape(values.shape)


def rounded(values):
    return values.astype(bf16).astype(f32)


def widen(values):
    return jnp.concatenate([values] * (WIDE // 128), axis=-1)


def norm_terms(total, square, count):
    mean = by_image(total) / count
    scaling = lax.rsqrt(by_image(square) / count - mean * mean + eps_norm)
    return (mean, scaling)


def main_kernel(
    pairs,
    strip_count,
    slots,
    slot_ref,
    place_ref,
    size_ref,
    strips_ref,
    goal_ref,
    gathered_ref,
    vec_two_ref,
    vec_hid_two_ref,
    vec_three_ref,
    vec_hid_three_ref,
    result_ref,
    pixel_ref,
    grad_ref,
    strips,
    line_tmp,
    x_ref,
    inv_ref,
    col_ref,
    pool_ref,
    mix_ref,
    zed_ref,
    dx_ref,
    u_ref,
    g_ref,
    h_ref,
    dy_ref,
    patch_ref,
    dpatch_ref,
    inv3_ref,
    e_ref,
    col3_ref,
    pool3_ref,
    mix3_ref,
    dx3_ref,
    u3_ref,
    g3_ref,
    h3_ref,
    dy3_ref,
    dpre_ref,
    w1_ref,
    w2_ref,
    we_ref,
    w3_ref,
    w4_ref,
    gw1_ref,
    gw2_ref,
    gwe_ref,
    gw3_ref,
    gw4_ref,
    acc_two,
    acc_hid_two,
    acc_three,
    acc_hid_three,
    flat_ref,
    in_sem,
    out_sem,
):
    pair = pl.program_id(0)
    weights = [w1_ref, w2_ref, we_ref, w3_ref, w4_ref]
    grads = [gw1_ref, gw2_ref, gwe_ref, gw3_ref, gw4_ref]

    def strip_copies(outward):
        copies = []
        for half in range(4):
            start = lax.rem(pair * 8 + strip_count - 2 + 2 * half, strip_count)
            inside = strips.at[pl.ds(2 * half, 2)]
            if outward:
                copies.append(
                    pltpu.make_async_copy(inside, pixel_ref.at[pl.ds(start, 2)], out_sem.at[half])
                )
            else:
                copies.append(
                    pltpu.make_async_copy(strips_ref.at[pl.ds(start, 2)], inside, in_sem.at[half])
                )
        return copies

    for copy in strip_copies(False):
        copy.start()

    left_half = lax.broadcasted_iota(jnp.int32, (HALF, 128), 1) < BS

    def unpack():
        offset = 0
        for (rows, cols), ref in zip(SHAPES, weights):
            wide = cols // BS
            for rb in range(rows // BS):
                for cb in range(0, wide, 2):
                    number = offset + rb * wide + cb
                    first = gathered_ref[slot_ref[number]].astype(f32)
                    turned = pltpu.roll(first, BS, 1)
                    if cb + 1 < wide:
                        second = gathered_ref[slot_ref[number + 1]].astype(f32)
                        top = jnp.where(left_half, first, pltpu.roll(second, BS, 1))
                        low = jnp.where(left_half, turned, second)
                    else:
                        top = jnp.where(left_half, first, 0.0)
                        low = jnp.where(left_half, turned, 0.0)
                    place = slice(cb * BS, cb * BS + 128)
                    ref[rb * BS : rb * BS + HALF, place] = top.astype(bf16)
                    ref[rb * BS + HALF : rb * BS + BS, place] = low.astype(bf16)
            offset += rows // BS * wide
        w3_ref[C3:, :] = jnp.zeros((WIDE - C3, HID3), bf16)

    @pl.when(pair == 0)
    def _():
        unpack()
        acc_two[...] = jnp.zeros(acc_two.shape, f32)
        acc_hid_two[...] = jnp.zeros(acc_hid_two.shape, f32)
        acc_three[...] = jnp.zeros(acc_three.shape, f32)
        acc_hid_three[...] = jnp.zeros(acc_hid_three.shape, f32)

    parity = lax.broadcasted_iota(jnp.int32, (8, 128), 0) % 2
    high = jnp.where(parity == 0, size_ref[pair * 4], size_ref[pair * 4 + 2])
    broad = jnp.where(parity == 0, size_ref[pair * 4 + 1], size_ref[pair * 4 + 3])
    count_two = (high * broad * C2).astype(f32)[:, :1]
    high3 = (high + 1) // 2
    broad3 = (broad + 1) // 2
    count_three = (high3 * broad3 * C3).astype(f32)[:, :1]
    place = lax.broadcasted_iota(jnp.int32, (LINE, 128), 0) // 2
    inside = lax.broadcasted_iota(jnp.int32, (LINE, 128), 0) < 2 * W3
    reach = []
    col_share = []
    for pc in range(2):
        column = 2 * place + pc
        reach.append(jnp.where(inside & (column < line(broad)), line(high), 0))
        edge = (column == 0) | (column == line(broad) - 1)
        col_share.append(jnp.where(edge, 0.5, 1.0 / 3.0))
    reach3 = jnp.where(inside & (place < line(broad3)), line(high3), 0)
    edge3 = (place == 0) | (place == line(broad3) - 1)
    col_share3 = jnp.where(edge3, 0.5, 1.0 / 3.0)

    def row_share(row, height):
        return jnp.where((row == 0) | (row == height - 1), 0.5, 1.0 / 3.0)

    gain1, bias1, scale1 = (vec_two_ref[n : n + 1] for n in range(3))
    gain2, bias2, scale2, out_bias = (vec_two_ref[n : n + 1] for n in range(3, 7))
    embed_bias, gain3, bias3, scale3 = (vec_three_ref[n : n + 1] for n in range(4))
    gain4, bias4, scale4, out_bias3 = (vec_three_ref[n : n + 1] for n in range(4, 8))

    for copy in strip_copies(False):
        copy.wait()

    zero_line = jnp.zeros((1, LINE, C2), f32)
    zero_line3 = jnp.zeros((1, LINE, WIDE), f32)
    for plane in range(4):
        col_ref[plane, 0:1] = zero_line
        col_ref[plane, H3 + 1 : H3 + 2] = zero_line
        zed_ref[plane, 0:1] = zero_line
    col3_ref[0:1] = zero_line3
    col3_ref[H3 + 1 : H3 + 2] = zero_line3

    def arrange(r, carry):
        total, square = carry
        for pr in range(2):
            row = 2 * r + pr
            strip = row // SR
            within = row - strip * SR
            for image in range(2):
                spot = pr * 2 + image
                line_tmp[spot, 0:CW] = strips[image * STRIPS + strip, within].astype(f32)
                for pc in range(2):
                    x_ref[pr * 2 + pc, r, pl.ds(image, W3, stride=2)] = line_tmp[
                        spot, pl.ds(pc, W3, stride=2)
                    ]
            for pc in range(2):
                plane = pr * 2 + pc
                valid = row < reach[pc]
                inv_ref[plane, r] = jnp.where(
                    valid, line(row_share(row, high)) * col_share[pc], 0.0
                )
                values = jnp.where(valid, x_ref[plane, r], 0.0)
                x_ref[plane, r] = values
                total = total + fold(values)
                square = square + fold(values * values)
        inv3_ref[r] = jnp.where(r < reach3, line(row_share(r, high3)) * col_share3, 0.0)
        return (total, square)

    nothing = jnp.zeros((8, C2), f32)
    nothing3 = jnp.zeros((8, WIDE), f32)
    total, square = lax.fori_loop(0, H3, arrange, (nothing, nothing))
    mean1, scaling1 = norm_terms(total, square, count_two)
    factor1 = line(scaling1 * gain1)
    shift1 = line(bias1 - mean1 * scaling1 * gain1)

    def window_cols(k, carry):
        rows = pl.ds(2 * k, 2)
        for pr in range(2):
            masked = []
            for pc in range(2):
                plane = pr * 2 + pc
                normal = rounded(x_ref[plane, rows] * factor1 + shift1)
                masked.append(jnp.where(inv_ref[plane, rows] > 0.0, normal, 0.0))
            both = masked[0] + masked[1]
            col_ref[pr * 2, pl.ds(2 * k + 1, 2)] = both + from_left(masked[1])
            col_ref[pr * 2 + 1, pl.ds(2 * k + 1, 2)] = both + from_right(masked[0])
        return carry

    lax.fori_loop(0, H3 // 2, window_cols, 0)

    def row_windows(pc, k):
        even = col_ref[pc, pl.ds(2 * k + 1, 2)]
        odd = col_ref[2 + pc, pl.ds(2 * k + 1, 2)]
        both = even + odd
        return (both + col_ref[2 + pc, pl.ds(2 * k, 2)], both + col_ref[pc, pl.ds(2 * k + 2, 2)])

    def mix(k, carry):
        total, square = carry
        rows = pl.ds(2 * k, 2)
        for pc in range(2):
            windows = row_windows(pc, k)
            for pr in range(2):
                plane = pr * 2 + pc
                values = x_ref[plane, rows]
                share = inv_ref[plane, rows]
                pooled = windows[pr] * share - rounded(values * factor1 + shift1)
                pooled = jnp.where(share > 0.0, pooled, 0.0)
                mixed = values + scale1 * pooled
                pool_ref[plane, rows] = pooled
                mix_ref[plane, rows] = mixed
                total = total + fold(mixed)
                square = square + fold(mixed * mixed)
        return (total, square)

    total, square = lax.fori_loop(0, H3 // 2, mix, (nothing, nothing))
    mean2, scaling2 = norm_terms(total, square, count_two)
    factor2 = line(scaling2 * gain2)
    shift2 = line(bias2 - mean2 * scaling2 * gain2)

    def where_chunk(c):
        plane = c // STEPS
        first = (c - plane * STEPS) * ROWS
        return (plane, first, pl.ds(pl.multiple_of(c * CHUNK, CHUNK), CHUNK))

    def branch(c, carry):
        plane, first, flat = where_chunk(c)
        mixed = mix_ref[plane, pl.ds(first, ROWS)]
        low = (mixed * factor2 + shift2).reshape(CHUNK, C2).astype(bf16)
        h_ref[flat] = low
        hidden = product(low, w1_ref[...]) + vec_hid_two_ref[...]
        active, slope = gelu_pair(hidden)
        active = active.astype(bf16)
        u_ref[flat] = active
        g_ref[flat] = slope.astype(bf16)
        out = (product(active, w2_ref[...]) + out_bias).reshape(ROWS, LINE, C2)
        valid = inv_ref[plane, pl.ds(first, ROWS)] > 0.0
        zed = rounded(jnp.where(valid, mixed + scale2 * out, 0.0))
        zed_ref[plane, pl.ds(first + 1, ROWS)] = zed
        return carry

    lax.fori_loop(0, 4 * STEPS, branch, 0)

    def patches(k, carry):
        flat = pl.ds(pl.multiple_of(k * 2 * LINE, 2 * LINE), 2 * LINE)
        for ky in range(3):
            pr = (0 if ky == 1 else 1) * 2
            rows = pl.ds(2 * k + (0 if ky == 0 else 1), 2)
            even = zed_ref[pr, rows]
            odd = zed_ref[pr + 1, rows]
            for kx, tap in enumerate((from_left(odd), even, odd)):
                at = (3 * ky + kx) * C2
                patch_ref[flat, at : at + C2] = tap.reshape(2 * LINE, C2).astype(bf16)
        return carry

    lax.fori_loop(0, H3 // 2, patches, 0)

    def embed(c, carry):
        total, square = carry
        flat = pl.ds(pl.multiple_of(c * CHUNK, CHUNK), CHUNK)
        rows = pl.ds(c * ROWS, ROWS)
        out = (product(patch_ref[flat], we_ref[...]) + embed_bias).reshape(ROWS, LINE, WIDE)
        out = jnp.where(widen(inv3_ref[rows]) > 0.0, out, 0.0)
        e_ref[rows] = out
        return (total + fold(out), square + fold(out * out))

    total, square = lax.fori_loop(0, STEPS, embed, (nothing3, nothing3))
    mean3, scaling3 = norm_terms(total, square, count_three)
    factor3 = line(scaling3 * gain3)
    shift3 = line(bias3 - mean3 * scaling3 * gain3)

    def window_cols3(k, carry):
        rows = pl.ds(2 * k, 2)
        normal = rounded(e_ref[rows] * factor3 + shift3)
        masked = jnp.where(widen(inv3_ref[rows]) > 0.0, normal, 0.0)
        col3_ref[pl.ds(2 * k + 1, 2)] = masked + from_left(masked) + from_right(masked)
        return carry

    lax.fori_loop(0, H3 // 2, window_cols3, 0)

    def row_windows3(k):
        return (
            col3_ref[pl.ds(2 * k, 2)]
            + col3_ref[pl.ds(2 * k + 1, 2)]
            + col3_ref[pl.ds(2 * k + 2, 2)]
        )

    def mix3(k, carry):
        total, square = carry
        rows = pl.ds(2 * k, 2)
        values = e_ref[rows]
        share = widen(inv3_ref[rows])
        pooled = row_windows3(k) * share - rounded(values * factor3 + shift3)
        pooled = jnp.where(share > 0.0, pooled, 0.0)
        mixed = values + scale3 * pooled
        pool3_ref[rows] = pooled
        mix3_ref[rows] = mixed
        return (total + fold(mixed), square + fold(mixed * mixed))

    total, square = lax.fori_loop(0, H3 // 2, mix3, (nothing3, nothing3))
    mean4, scaling4 = norm_terms(total, square, count_three)
    factor4 = line(scaling4 * gain4)
    shift4 = line(bias4 - mean4 * scaling4 * gain4)
    normal4 = (spread(scaling4, WIDE), spread(-mean4 * scaling4, WIDE))

    def branch3(c, carry):
        d_out_bias, d_scale, d_hidden_bias, d_shift, d_gain = carry
        flat = pl.ds(pl.multiple_of(c * CHUNK, CHUNK), CHUNK)
        rows = pl.ds(c * ROWS, ROWS)
        mixed = mix3_ref[rows]
        low = (mixed * factor4 + shift4).reshape(CHUNK, WIDE).astype(bf16)
        h3_ref[flat] = low
        hidden = product(low, w3_ref[...]) + vec_hid_three_ref[...]
        active, slope = gelu_pair(hidden)
        active = active.astype(bf16)
        u3_ref[flat] = active
        out = (product(active, w4_ref[...]) + out_bias3).reshape(ROWS, LINE, WIDE)
        valid = widen(inv3_ref[rows]) > 0.0
        out = jnp.where(valid, out, 0.0)
        result_ref[0, rows] = mixed + scale4 * out
        goal = jnp.where(valid, goal_ref[0, flat].astype(f32).reshape(ROWS, LINE, WIDE), 0.0)
        low_goal = (scale4 * goal).reshape(CHUNK, WIDE).astype(bf16)
        dy3_ref[flat] = low_goal
        d_hidden = (slope * product_nt(low_goal, w4_ref[...])).astype(bf16)
        g3_ref[flat] = d_hidden
        d_low = product_nt(d_hidden, w3_ref[...]).reshape(ROWS, LINE, WIDE)
        dx3_ref[rows] = d_low
        normal = mixed * normal4[0] + normal4[1]
        return (
            d_out_bias + fold(low_goal.astype(f32)),
            d_scale + fold(out * goal),
            d_hidden_bias + fold(d_hidden.astype(f32)),
            d_shift + fold(d_low),
            d_gain + fold(d_low * normal),
        )

    wide_zero = jnp.zeros((8, HID3), f32)
    d_out_bias, d_scale, d_hidden_bias, d_shift, d_gain = lax.fori_loop(
        0, STEPS, branch3, (nothing3, nothing3, wide_zero, nothing3, nothing3)
    )
    acc_three[7] += d_out_bias
    acc_three[6] += d_scale
    acc_hid_three[...] += d_hidden_bias
    acc_three[5] += d_shift
    acc_three[4] += d_gain
    mean_shift = by_image(d_shift * gain4) / count_three
    mean_gain = by_image(d_gain * gain4) / count_three

    def keep(ref, value):
        if pairs == 1:
            ref[...] = value
        else:

            @pl.when(pair == 0)
            def _():
                ref[...] = value

            @pl.when(pair > 0)
            def _():
                ref[...] += value

    keep(gw3_ref, product_tn(h3_ref[...], g3_ref[...]))
    keep(gw4_ref, product_tn(u3_ref[...], dy3_ref[...]))

    back_gain4 = line(scaling4 * gain4)
    back_mean4 = spread(scaling4 * mean_shift, WIDE)
    back_normal4 = spread(scaling4 * mean_gain, WIDE)

    def unmix3(k, d_scale):
        rows = pl.ds(2 * k, 2)
        flat = pl.ds(pl.multiple_of(k * 2 * LINE, 2 * LINE), 2 * LINE)
        share = widen(inv3_ref[rows])
        valid = share > 0.0
        normal = mix3_ref[rows] * normal4[0] + normal4[1]
        back = dx3_ref[rows] * back_gain4 - back_mean4 - normal * back_normal4
        goal = goal_ref[0, flat].astype(f32).reshape(2, LINE, WIDE)
        d_mixed = jnp.where(valid, back + goal, 0.0)
        dx3_ref[rows] = d_mixed
        d_scale = d_scale + fold(pool3_ref[rows] * d_mixed)
        weighted = scale3 * d_mixed * share
        col3_ref[pl.ds(2 * k + 1, 2)] = weighted + from_left(weighted) + from_right(weighted)
        return d_scale

    acc_three[3] += lax.fori_loop(0, H3 // 2, unmix3, nothing3)
    normal3 = (spread(scaling3, WIDE), spread(-mean3 * scaling3, WIDE))

    def unpool3(k, carry):
        d_shift, d_gain = carry
        rows = pl.ds(2 * k, 2)
        valid = widen(inv3_ref[rows]) > 0.0
        d_normal = jnp.where(valid, row_windows3(k) - scale3 * dx3_ref[rows], 0.0)
        pool3_ref[rows] = d_normal
        normal = e_ref[rows] * normal3[0] + normal3[1]
        return (d_shift + fold(d_normal), d_gain + fold(d_normal * normal))

    d_shift, d_gain = lax.fori_loop(0, H3 // 2, unpool3, (nothing3, nothing3))
    acc_three[2] += d_shift
    acc_three[1] += d_gain
    mean_shift = by_image(d_shift * gain3) / count_three
    mean_gain = by_image(d_gain * gain3) / count_three
    back_gain3 = line(scaling3 * gain3)
    back_mean3 = spread(scaling3 * mean_shift, WIDE)
    back_normal3 = spread(scaling3 * mean_gain, WIDE)

    def unnorm3(k, d_bias):
        rows = pl.ds(2 * k, 2)
        flat = pl.ds(pl.multiple_of(k * 2 * LINE, 2 * LINE), 2 * LINE)
        valid = widen(inv3_ref[rows]) > 0.0
        normal = e_ref[rows] * normal3[0] + normal3[1]
        back = pool3_ref[rows] * back_gain3 - back_mean3 - normal * back_normal3
        low = jnp.where(valid, dx3_ref[rows] + back, 0.0).astype(bf16)
        dpre_ref[flat] = low.reshape(2 * LINE, WIDE)
        return d_bias + fold(low.astype(f32))

    acc_three[0] += lax.fori_loop(0, H3 // 2, unnorm3, nothing3)
    keep(gwe_ref, product_tn(patch_ref[...], dpre_ref[...]))

    def unpatch(c, carry):
        flat = pl.ds(pl.multiple_of(c * CHUNK, CHUNK), CHUNK)
        rows = pl.ds(c * ROWS, ROWS)
        dpatch_ref[rows] = product_nt(dpre_ref[flat], we_ref[...]).reshape(ROWS, LINE, 9 * C2)
        return carry

    lax.fori_loop(0, STEPS, unpatch, 0)
    dpatch_ref[H3 : H3 + 1] = jnp.zeros((1, LINE, 9 * C2), f32)

    def tap(ky, kx, rows):
        at = (3 * ky + kx) * C2
        return dpatch_ref[rows, :, at : at + C2]

    def gather_back(k, carry):
        here = pl.ds(2 * k, 2)
        below = pl.ds(2 * k + 1, 2)
        sources = []
        for ky, rows in ((0, below), (1, here), (2, here)):
            sources.append((tap(ky, 1, rows), tap(ky, 2, rows) + from_right(tap(ky, 0, rows))))
        for pc in range(2):
            for pr, value in ((0, sources[1][pc]), (1, sources[2][pc] + sources[0][pc])):
                plane = pr * 2 + pc
                valid = inv_ref[plane, here] > 0.0
                zed_ref[plane, here] = jnp.where(valid, rounded(value), 0.0)
        return carry

    lax.fori_loop(0, H3 // 2, gather_back, 0)

    normal2 = (spread(scaling2, C2), spread(-mean2 * scaling2, C2))

    def unbranch(c, carry):
        d_out_bias, d_hidden_bias, d_shift, d_gain = carry
        plane, first, flat = where_chunk(c)
        rows = pl.ds(first, ROWS)
        low_goal = (scale2 * zed_ref[plane, rows]).reshape(CHUNK, C2).astype(bf16)
        dy_ref[flat] = low_goal
        d_hidden = g_ref[flat].astype(f32) * product_nt(low_goal, w2_ref[...])
        d_hidden = d_hidden.astype(bf16)
        g_ref[flat] = d_hidden
        d_low = product_nt(d_hidden, w1_ref[...]).reshape(ROWS, LINE, C2)
        dx_ref[plane, rows] = d_low
        normal = mix_ref[plane, rows] * normal2[0] + normal2[1]
        return (
            d_out_bias + fold(low_goal.astype(f32)),
            d_hidden_bias + fold(d_hidden.astype(f32)),
            d_shift + fold(d_low),
            d_gain + fold(d_low * normal),
        )

    d_out_bias, d_hidden_bias, d_shift, d_gain = lax.fori_loop(
        0, 4 * STEPS, unbranch, (nothing, jnp.zeros((8, HID2), f32), nothing, nothing)
    )
    acc_two[6] += d_out_bias
    acc_hid_two[...] += d_hidden_bias
    acc_two[4] += d_shift
    acc_two[3] += d_gain
    mean_shift = by_image(d_shift * gain2) / count_two
    mean_gain = by_image(d_gain * gain2) / count_two
    keep(gw1_ref, product_tn(h_ref[...], g_ref[...]))
    new_gw2 = product_tn(dy_ref[...], u_ref[...]).T
    keep(gw2_ref, new_gw2)
    d_scale = fold(w2_ref[...].astype(f32) * new_gw2) + out_bias * d_out_bias
    acc_two[5] += d_scale / scale2

    back_gain2 = line(scaling2 * gain2)
    back_mean2 = spread(scaling2 * mean_shift, C2)
    back_normal2 = spread(scaling2 * mean_gain, C2)

    def unmix(k, d_scale):
        rows = pl.ds(2 * k, 2)
        for pr in range(2):
            weighted = []
            for pc in range(2):
                plane = pr * 2 + pc
                share = inv_ref[plane, rows]
                normal = mix_ref[plane, rows] * normal2[0] + normal2[1]
                back = dx_ref[plane, rows] * back_gain2 - back_mean2 - normal * back_normal2
                d_mixed = jnp.where(share > 0.0, zed_ref[plane, rows] + back, 0.0)
                dx_ref[plane, rows] = d_mixed
                d_scale = d_scale + fold(pool_ref[plane, rows] * d_mixed)
                weighted.append(scale1 * d_mixed * share)
            both = weighted[0] + weighted[1]
            col_ref[pr * 2, pl.ds(2 * k + 1, 2)] = both + from_left(weighted[1])
            col_ref[pr * 2 + 1, pl.ds(2 * k + 1, 2)] = both + from_right(weighted[0])
        return d_scale

    acc_two[2] += lax.fori_loop(0, H3 // 2, unmix, nothing)
    normal1 = (spread(scaling1, C2), spread(-mean1 * scaling1, C2))

    def unpool(k, carry):
        d_shift, d_gain = carry
        rows = pl.ds(2 * k, 2)
        for pc in range(2):
            windows = row_windows(pc, k)
            for pr in range(2):
                plane = pr * 2 + pc
                valid = inv_ref[plane, rows] > 0.0
                d_normal = windows[pr] - scale1 * dx_ref[plane, rows]
                d_normal = jnp.where(valid, d_normal, 0.0)
                pool_ref[plane, rows] = d_normal
                normal = x_ref[plane, rows] * normal1[0] + normal1[1]
                d_shift = d_shift + fold(d_normal)
                d_gain = d_gain + fold(d_normal * normal)
        return (d_shift, d_gain)

    d_shift, d_gain = lax.fori_loop(0, H3 // 2, unpool, (nothing, nothing))
    acc_two[1] += d_shift
    acc_two[0] += d_gain
    mean_shift = by_image(d_shift * gain1) / count_two
    mean_gain = by_image(d_gain * gain1) / count_two
    back_gain1 = line(scaling1 * gain1)
    back_mean1 = spread(scaling1 * mean_shift, C2)
    back_normal1 = spread(scaling1 * mean_gain, C2)

    def unnorm(r, carry):
        for pr in range(2):
            row = 2 * r + pr
            strip = row // SR
            within = row - strip * SR
            for pc in range(2):
                plane = pr * 2 + pc
                normal = x_ref[plane, r] * normal1[0] + normal1[1]
                back = pool_ref[plane, r] * back_gain1 - back_mean1 - normal * back_normal1
                dx_ref[plane, r] = jnp.where(
                    inv_ref[plane, r] > 0.0, dx_ref[plane, r] + back, 0.0
                )
            for image in range(2):
                spot = pr * 2 + image
                for pc in range(2):
                    line_tmp[spot, pl.ds(pc, W3, stride=2)] = dx_ref[
                        pr * 2 + pc, r, pl.ds(image, W3, stride=2)
                    ]
                strips[image * STRIPS + strip, within] = line_tmp[spot, 0:CW].astype(bf16)
        return carry

    lax.fori_loop(0, H3, unnorm, 0)
    for copy in strip_copies(True):
        copy.start()

    @pl.when(pair == pairs - 1)
    def _():
        offset = 0
        for (rows, cols), ref in zip(SHAPES, grads):
            wide = cols // BS
            for rb in range(rows // BS):
                for cb in range(0, wide, 2):
                    number = offset + rb * wide + cb
                    at = slice(cb * BS, cb * BS + 128)
                    top = ref[rb * BS : rb * BS + HALF, at]
                    low = ref[rb * BS + HALF : rb * BS + BS, at]
                    grad_ref[place_ref[number]] = jnp.where(
                        left_half, top, pltpu.roll(low, BS, 1)
                    ).astype(bf16)
                    if cb + 1 < wide:
                        grad_ref[place_ref[number + 1]] = jnp.where(
                            left_half, pltpu.roll(top, BS, 1), low
                        ).astype(bf16)
            offset += rows // BS * wide

        def filler(number, carry):
            grad_ref[place_ref[number]] = jnp.zeros((HALF, 128), bf16)
            return carry

        lax.fori_loop(USED, slots, filler, 0)

        flat_ref[...] = jnp.zeros(flat_ref.shape, f32)

        def put(at, total, length):
            if at % 128:
                room = jnp.zeros((8, 128), f32)
                if total.shape[1] < length + BS:
                    total = jnp.concatenate([total, room], axis=1)
                total = pltpu.roll(total, BS, 1)
            whole = jnp.sum(total, axis=0, keepdims=True)
            done = -(at % 128)
            row = at // 128
            lane = 0
            while done < length:
                first = max(0, -done)
                last = min(128, length - done)
                flat_ref[row : row + 1, first:last] = whole[:, lane + first : lane + last]
                done += 128
                lane += 128
                row += 1

        at = 0
        for n in range(6):
            put(at, acc_two[n], C2)
            at += C2
        put(at, acc_hid_two[...], HID2)
        at += HID2
        put(at, acc_two[6], C2)
        at += C2
        for n in range(7):
            put(at, acc_three[n], C3)
            at += C3
        put(at, acc_hid_three[...], HID3)
        at += HID3
        put(at, acc_three[7], C3)
        packed = flat_ref[...].astype(bf16)
        stride = slots // strip_count + EXTRA
        for n in range(EXTRA):
            piece = packed[n * HALF : (n + 1) * HALF]

            def leave(target, carry):
                grad_ref[target * stride + stride - EXTRA + n] = piece
                return carry

            lax.fori_loop(0, strip_count, leave, 0)

    for copy in strip_copies(True):
        copy.wait()


def run_main(slot_of, place_of, sizes, strips, goal, gathered, vec_two, vec_hid_two, vec_three, vec_hid_three):
    strip_count = strips.shape[0]
    pairs = goal.shape[0]
    slots = gathered.shape[0]
    rows_out = slots + EXTRA * strip_count

    def whole(shape):
        return pl.BlockSpec(shape, lambda t: (0,) * len(shape), pipeline_mode=pl.Buffered(1))

    smem = pl.BlockSpec(memory_space=pltpu.SMEM)
    anywhere = pl.BlockSpec(memory_space=pl.ANY)
    plane_f32 = pltpu.VMEM((4, H3, LINE, C2), f32)
    wide_f32 = pltpu.VMEM((H3, LINE, WIDE), f32)
    scratch = [
        pltpu.VMEM((2 * STRIPS, SR, CW, C2), bf16),
        pltpu.VMEM((4, LINE, C2), f32),
        plane_f32,
        plane_f32,
        pltpu.VMEM((4, H3 + 2, LINE, C2), f32),
        plane_f32,
        plane_f32,
        pltpu.VMEM((4, H3 + 1, LINE, C2), f32),
        plane_f32,
        pltpu.VMEM((4 * PLANE, HID2), bf16),
        pltpu.VMEM((4 * PLANE, HID2), bf16),
        pltpu.VMEM((4 * PLANE, C2), bf16),
        pltpu.VMEM((4 * PLANE, C2), bf16),
        pltpu.VMEM((PLANE, 9 * C2), bf16),
        pltpu.VMEM((H3 + 1, LINE, 9 * C2), f32),
        pltpu.VMEM((H3, LINE, 128), f32),
        wide_f32,
        pltpu.VMEM((H3 + 2, LINE, WIDE), f32),
        wide_f32,
        wide_f32,
        wide_f32,
        pltpu.VMEM((PLANE, HID3), bf16),
        pltpu.VMEM((PLANE, HID3), bf16),
        pltpu.VMEM((PLANE, WIDE), bf16),
        pltpu.VMEM((PLANE, WIDE), bf16),
        pltpu.VMEM((PLANE, WIDE), bf16),
        pltpu.VMEM((C2, HID2), bf16),
        pltpu.VMEM((HID2, C2), bf16),
        pltpu.VMEM((9 * C2, WIDE), bf16),
        pltpu.VMEM((WIDE, HID3), bf16),
        pltpu.VMEM((HID3, WIDE), bf16),
        pltpu.VMEM((C2, HID2), f32),
        pltpu.VMEM((HID2, C2), f32),
        pltpu.VMEM((9 * C2, WIDE), f32),
        pltpu.VMEM((WIDE, HID3), f32),
        pltpu.VMEM((HID3, WIDE), f32),
        pltpu.VMEM((7, 8, C2), f32),
        pltpu.VMEM((8, HID2), f32),
        pltpu.VMEM((8, 8, WIDE), f32),
        pltpu.VMEM((8, HID3), f32),
        pltpu.VMEM((EXTRA * HALF, 128), f32),
        pltpu.SemaphoreType.DMA((4,)),
        pltpu.SemaphoreType.DMA((4,)),
    ]
    return pl.pallas_call(
        functools.partial(main_kernel, pairs, strip_count, slots),
        grid=(pairs,),
        in_specs=[
            smem,
            smem,
            smem,
            anywhere,
            pl.BlockSpec((1,) + goal.shape[1:], lambda t: (t, 0, 0)),
            whole(gathered.shape),
            whole(vec_two.shape),
            whole(vec_hid_two.shape),
            whole(vec_three.shape),
            whole(vec_hid_three.shape),
        ],
        out_specs=[
            pl.BlockSpec((1, H3, LINE, WIDE), lambda t: (t, 0, 0, 0)),
            anywhere,
            whole((rows_out, HALF, 128)),
        ],
        out_shape=[
            jax.ShapeDtypeStruct((pairs, H3, LINE, WIDE), f32),
            jax.ShapeDtypeStruct(strips.shape, bf16),
            jax.ShapeDtypeStruct((rows_out, HALF, 128), bf16),
        ],
        scratch_shapes=scratch,
        compiler_params=pltpu.CompilerParams(vmem_limit_bytes=62 * 1024 * 1024),
        name="blocks",
    )(slot_of, place_of, sizes, strips, goal, gathered, vec_two, vec_hid_two, vec_three, vec_hid_three)


def pack_kernel(master_ref, dense_ref):
    values = master_ref[...]
    dense_ref[...] = jnp.concatenate([values[:, :HALF], values[:, HALF:]], axis=2).astype(bf16)


def pack(master):
    owned = master.shape[0]
    return pl.pallas_call(
        pack_kernel,
        out_shape=jax.ShapeDtypeStruct((owned, HALF, 2 * BS), bf16),
        name="pack",
    )(master)


def update_kernel(
    factor_ref,
    summed_ref,
    master_ref,
    left_stat_ref,
    right_stat_ref,
    left_root_ref,
    right_root_ref,
    grad_ref,
    left_ref,
    right_ref,
    new_ref,
    copy_ref,
):
    factor = factor_ref[0]

    def one(n, carry):
        dense = summed_ref[n] * factor
        grad = jnp.concatenate([dense[:, :BS], dense[:, BS:]], axis=0)
        grad_ref[n] = grad
        low = grad.astype(bf16)
        left_ref[n] = 0.5 * left_stat_ref[n] + 0.5 * product_nt(low, low)
        right_ref[n] = 0.5 * right_stat_ref[n] + 0.5 * product_tn(low, low)
        stepped = product(left_root_ref[n].astype(bf16), low).astype(bf16)
        stepped = product(stepped, right_root_ref[n].astype(bf16))
        new = master_ref[n] - rate_matrix * stepped
        new_ref[n] = new
        copy_ref[n] = new.astype(bf16)
        return carry

    lax.fori_loop(0, grad_ref.shape[0], one, 0)


def update(factor, summed, master, left_stat, right_stat, left_root, right_root):
    owned = master.shape[0]
    part = min(owned, 7)
    square = pl.BlockSpec((part, BS, BS), lambda t: (t, 0, 0))
    shape = jax.ShapeDtypeStruct(master.shape, f32)
    return pl.pallas_call(
        update_kernel,
        grid=(-(-owned // part),),
        in_specs=[
            pl.BlockSpec(memory_space=pltpu.SMEM),
            pl.BlockSpec((part, HALF, 2 * BS), lambda t: (t, 0, 0)),
        ]
        + [square] * 5,
        out_specs=[square] * 5,
        out_shape=[shape] * 4 + [jax.ShapeDtypeStruct(master.shape, bf16)],
        name="update",
    )(factor, summed, master, left_stat, right_stat, left_root, right_root)


def share_out(pieces, axis):
    return lax.all_to_all(pieces, axis, split_axis=0, concat_axis=0, tiled=True)


def to_all(piece, axis):
    count = lax.axis_size(axis)
    return share_out(jnp.broadcast_to(piece[None], (count,) + piece.shape), axis)


def on_device(
    pixels,
    buckets,
    slot_owner_table,
    out_grad,
    master,
    left_stat,
    right_stat,
    left_root,
    right_root,
    vectors,
    moment,
):
    tile_count = lax.axis_size("tile")
    tile_place = lax.axis_index("tile")
    slot_count = pixels.shape[2]
    group_count = tile_count // STRIPS
    pairs = group_count // 2
    owned = master.shape[0]
    slots = owned * tile_count
    strips = share_out(pixels.reshape((tile_count,) + pixels.shape[3:]), "tile")
    gathered = lax.all_gather(pack(master), "tile", axis=0, tiled=True)

    numbers = jnp.arange(slots, dtype=jnp.int32)
    slot_of = jnp.sum(
        jnp.where(slot_owner_table[None, :] == numbers[:, None], numbers[None, :], 0), axis=1
    )
    place_of = slot_of + EXTRA * (slot_of // owned)
    image_ids = lax.dynamic_index_in_dim(
        buckets.reshape(group_count, slot_count), tile_place, 1, keepdims=False
    )
    heights = jnp.where(image_ids == 0, 5 * CH // 9, jnp.where(image_ids == 1, 7 * CH // 9, CH))
    breadths = jnp.where(image_ids == 0, CW, jnp.where(image_ids == 1, 7 * CW // 9, 5 * CW // 9))
    sizes = jnp.stack([heights, breadths], axis=1).reshape(-1).astype(jnp.int32)

    two = 6 * C2 + HID2 + C2
    vec_two = jnp.concatenate([vectors[: 6 * C2], vectors[6 * C2 + HID2 : two]]).reshape(7, C2)
    vec_hid_two = vectors[6 * C2 : 6 * C2 + HID2].reshape(1, HID2)
    wide_end = two + 7 * C3
    vec_three = jnp.concatenate([vectors[two:wide_end], vectors[wide_end + HID3 :]])
    vec_three = jnp.pad(vec_three.reshape(8, C3), ((0, 0), (0, WIDE - C3)))
    vec_hid_three = vectors[wide_end : wide_end + HID3].reshape(1, HID3)

    goal = out_grad.reshape(pairs, 2, H3, W3, C3).transpose(0, 2, 3, 1, 4)
    goal = goal.reshape(pairs, H3, 2 * W3, C3)
    goal = jnp.pad(goal, ((0, 0), (0, 0), (0, LINE - 2 * W3), (0, WIDE - C3)))
    goal = goal.reshape(pairs, PLANE, WIDE)

    result, pixel_back, outgoing = run_main(
        slot_of,
        place_of,
        sizes,
        strips,
        goal,
        gathered,
        vec_two,
        vec_hid_two,
        vec_three,
        vec_hid_three,
    )
    result = result[:, :, : 2 * W3, :C3].reshape(pairs, H3, W3, 2, C3).transpose(0, 3, 1, 2, 4)

    outgoing = outgoing.reshape(tile_count, owned + EXTRA, HALF, 128)
    tile_sum = jnp.sum(share_out(outgoing, "tile").astype(f32), axis=0)
    summed = jnp.sum(to_all(tile_sum.astype(bf16), "batch").astype(f32), axis=0)
    mine = summed[:owned]
    whole_vector = summed[owned:].reshape(-1)[: vectors.shape[0]]
    share = vectors.shape[0] // tile_count
    mine_vector = lax.dynamic_slice_in_dim(whole_vector, tile_place * share, share, 0)
    part = jnp.sum(mine * mine)
    square = jnp.sum(to_all(jnp.full((1, 128), part), "tile")[:, 0, 0])
    square = square + jnp.sum(whole_vector * whole_vector)
    clip_norm = jnp.sqrt(square)
    factor = jnp.minimum(1.0, clip_limit / clip_norm)
    block_grad, left_new, right_new, master_new, weight_copy = update(
        factor.reshape(1), mine, master, left_stat, right_stat, left_root, right_root
    )
    vec_grad = mine_vector * factor
    vec_moment = moment + vec_grad * vec_grad
    own_vectors = lax.dynamic_slice_in_dim(vectors, tile_place * share, share, 0)
    vec_new = own_vectors - rate_vector * vec_grad / (jnp.sqrt(vec_moment) + eps_adagrad)
    returned = share_out(pixel_back, "tile")
    return (
        result.reshape(out_grad.shape),
        returned.astype(f32).reshape(pixels.shape),
        clip_norm,
        block_grad,
        left_new,
        right_new,
        master_new,
        weight_copy,
        vec_grad,
        vec_moment,
        vec_new,
    )


def solution(mesh):
    placed = (
        P("batch", "tile", None, None, None, None),
        P("batch"),
        P(),
        P("batch", "tile", None, None, None, None, None),
        P("tile", None, None),
        P("tile", None, None),
        P("tile", None, None),
        P("tile", None, None),
        P("tile", None, None),
        P(),
        P("tile"),
    )
    return jax.shard_map(
        on_device,
        mesh=mesh,
        in_specs=placed,
        out_specs=(
            P("batch", "tile", None, None, None, None, None),
            P("batch", "tile", None, None, None, None),
            P(),
            P("tile", None, None),
            P("tile", None, None),
            P("tile", None, None),
            P("tile", None, None),
            P("tile", None, None),
            P("tile"),
            P("tile"),
            P("tile"),
        ),
        check_vma=False,
    )
```

```python
import functools

import jax
import jax.numpy as jnp
from jax import lax
from jax.experimental import pallas as pl
from jax.experimental.pallas import tpu as pltpu
from jax.sharding import PartitionSpec as P

C2 = 128
HID2 = 512
C3 = 320
HID3 = 1280
CH = 36
CW = 36
STRIPS = 4
BS = 64
SR = CH // STRIPS
H3 = CH // 2
W3 = CW // 2
WIDE = 384
LINE = 40
PLANE = H3 * LINE
ROWS = 6
CHUNK = ROWS * LINE
STEPS = H3 // ROWS
HALF = BS // 2

eps_norm = 1e-05
clip_limit = 1.0
rate_matrix = 0.3
rate_vector = 0.3
eps_adagrad = 1e-08
f32 = jnp.float32
bf16 = jnp.bfloat16

SHAPES = [(C2, HID2), (HID2, C2), (9 * C2, C3), (C3, HID3), (HID3, C3)]
USED = sum(rows // BS * (cols // BS) for rows, cols in SHAPES)
VEC_ROWS = (6 * C2 + HID2 + C2 + C3 + 6 * C3 + HID3 + C3) // 128


def extra_of(owned, groups):
    extra = -(-VEC_ROWS // HALF)
    return extra + -(owned + extra) % groups


def product(left, right):
    return jnp.dot(left, right, preferred_element_type=f32)


def product_nt(left, right):
    return lax.dot_general(left, right, (((1,), (1,)), ((), ())), preferred_element_type=f32)


def product_tn(left, right):
    return lax.dot_general(left, right, (((0,), (0,)), ((), ())), preferred_element_type=f32)


def gelu_pair(values):
    bell = jnp.exp2(values * values * (-0.5 * 1.4426950408889634))
    step = pl.reciprocal(1.0 + (0.3275911 * 0.7071067811865476) * jnp.abs(values), approx=True)
    tail = step * (
        0.5 * 0.254829592
        + step
        * (
            0.5 * -0.284496736
            + step
            * (0.5 * 1.421413741 + step * (0.5 * -1.453152027 + step * (0.5 * 1.061405429)))
        )
    )
    tail = tail * bell
    share = jnp.where(values >= 0.0, 1.0 - tail, tail)
    return (values * share, share + values * (bell * 0.3989422804014327))


def fold(values):
    chans = values.shape[-1]
    return jnp.sum(values.reshape(-1, 8, chans), axis=0)


def by_image(total):
    total = total + pltpu.roll(total, 4, 0)
    total = total + pltpu.roll(total, 2, 0)
    return jnp.sum(total, axis=1, keepdims=True)


def line(pattern):
    return jnp.concatenate([pattern] * (LINE // 8), axis=0)


def spread(pattern, chans):
    return line(jnp.broadcast_to(pattern, (8, chans)))


def from_left(values):
    flat = values.reshape(-1, values.shape[-1])
    return pltpu.roll(flat, 2, 0).reshape(values.shape)


def from_right(values):
    flat = values.reshape(-1, values.shape[-1])
    return pltpu.roll(flat, flat.shape[0] - 2, 0).reshape(values.shape)


def rounded(values):
    return values.astype(bf16).astype(f32)


def widen(values):
    return jnp.concatenate([values] * (WIDE // 128), axis=-1)


def norm_terms(total, square, count):
    mean = by_image(total) / count
    scaling = lax.rsqrt(by_image(square) / count - mean * mean + eps_norm)
    return (mean, scaling)


def main_kernel(
    pairs,
    strip_count,
    slots,
    extra,
    slot_ref,
    place_ref,
    size_ref,
    strips_ref,
    goal_ref,
    gathered_ref,
    vec_two_ref,
    vec_hid_two_ref,
    vec_three_ref,
    vec_hid_three_ref,
    result_ref,
    pixel_ref,
    grad_ref,
    strips,
    line_tmp,
    x_ref,
    inv_ref,
    col_ref,
    pool_ref,
    mix_ref,
    zed_ref,
    dx_ref,
    u_ref,
    g_ref,
    h_ref,
    dy_ref,
    patch_ref,
    dpatch_ref,
    inv3_ref,
    e_ref,
    col3_ref,
    pool3_ref,
    mix3_ref,
    dx3_ref,
    u3_ref,
    g3_ref,
    h3_ref,
    dy3_ref,
    dpre_ref,
    w1_ref,
    w2_ref,
    we_ref,
    w3_ref,
    w4_ref,
    gw1_ref,
    gw2_ref,
    gwe_ref,
    gw3_ref,
    gw4_ref,
    acc_two,
    acc_hid_two,
    acc_three,
    acc_hid_three,
    flat_ref,
    in_sem,
    out_sem,
):
    pair = pl.program_id(0)
    weights = [w1_ref, w2_ref, we_ref, w3_ref, w4_ref]
    grads = [gw1_ref, gw2_ref, gwe_ref, gw3_ref, gw4_ref]

    def strip_copies(outward):
        copies = []
        for half in range(4):
            start = lax.rem(pair * 8 + strip_count - 2 + 2 * half, strip_count)
            inside = strips.at[pl.ds(2 * half, 2)]
            if outward:
                copies.append(
                    pltpu.make_async_copy(inside, pixel_ref.at[pl.ds(start, 2)], out_sem.at[half])
                )
            else:
                copies.append(
                    pltpu.make_async_copy(strips_ref.at[pl.ds(start, 2)], inside, in_sem.at[half])
                )
        return copies

    for copy in strip_copies(False):
        copy.start()

    left_half = lax.broadcasted_iota(jnp.int32, (HALF, 128), 1) < BS

    def unpack():
        offset = 0
        for (rows, cols), ref in zip(SHAPES, weights):
            wide = cols // BS
            for rb in range(rows // BS):
                for cb in range(0, wide, 2):
                    number = offset + rb * wide + cb
                    first = gathered_ref[slot_ref[number]].astype(f32)
                    turned = pltpu.roll(first, BS, 1)
                    if cb + 1 < wide:
                        second = gathered_ref[slot_ref[number + 1]].astype(f32)
                        top = jnp.where(left_half, first, pltpu.roll(second, BS, 1))
                        low = jnp.where(left_half, turned, second)
                    else:
                        top = jnp.where(left_half, first, 0.0)
                        low = jnp.where(left_half, turned, 0.0)
                    place = slice(cb * BS, cb * BS + 128)
                    ref[rb * BS : rb * BS + HALF, place] = top.astype(bf16)
                    ref[rb * BS + HALF : rb * BS + BS, place] = low.astype(bf16)
            offset += rows // BS * wide
        w3_ref[C3:, :] = jnp.zeros((WIDE - C3, HID3), bf16)

    @pl.when(pair == 0)
    def _():
        unpack()
        acc_two[...] = jnp.zeros(acc_two.shape, f32)
        acc_hid_two[...] = jnp.zeros(acc_hid_two.shape, f32)
        acc_three[...] = jnp.zeros(acc_three.shape, f32)
        acc_hid_three[...] = jnp.zeros(acc_hid_three.shape, f32)

    parity = lax.broadcasted_iota(jnp.int32, (8, 128), 0) % 2
    high = jnp.where(parity == 0, size_ref[pair * 4], size_ref[pair * 4 + 2])
    broad = jnp.where(parity == 0, size_ref[pair * 4 + 1], size_ref[pair * 4 + 3])
    count_two = (high * broad * C2).astype(f32)[:, :1]
    high3 = (high + 1) // 2
    broad3 = (broad + 1) // 2
    count_three = (high3 * broad3 * C3).astype(f32)[:, :1]
    place = lax.broadcasted_iota(jnp.int32, (LINE, 128), 0) // 2
    inside = lax.broadcasted_iota(jnp.int32, (LINE, 128), 0) < 2 * W3
    reach = []
    col_share = []
    for pc in range(2):
        column = 2 * place + pc
        reach.append(jnp.where(inside & (column < line(broad)), line(high), 0))
        edge = (column == 0) | (column == line(broad) - 1)
        col_share.append(jnp.where(edge, 0.5, 1.0 / 3.0))
    reach3 = jnp.where(inside & (place < line(broad3)), line(high3), 0)
    edge3 = (place == 0) | (place == line(broad3) - 1)
    col_share3 = jnp.where(edge3, 0.5, 1.0 / 3.0)

    def row_share(row, height):
        return jnp.where((row == 0) | (row == height - 1), 0.5, 1.0 / 3.0)

    gain1, bias1, scale1 = (vec_two_ref[n : n + 1] for n in range(3))
    gain2, bias2, scale2, out_bias = (vec_two_ref[n : n + 1] for n in range(3, 7))
    embed_bias, gain3, bias3, scale3 = (vec_three_ref[n : n + 1] for n in range(4))
    gain4, bias4, scale4, out_bias3 = (vec_three_ref[n : n + 1] for n in range(4, 8))

    for copy in strip_copies(False):
        copy.wait()

    zero_line = jnp.zeros((1, LINE, C2), f32)
    zero_line3 = jnp.zeros((1, LINE, WIDE), f32)
    for plane in range(4):
        col_ref[plane, 0:1] = zero_line
        col_ref[plane, H3 + 1 : H3 + 2] = zero_line
        zed_ref[plane, 0:1] = zero_line
    col3_ref[0:1] = zero_line3
    col3_ref[H3 + 1 : H3 + 2] = zero_line3

    def arrange(r, carry):
        total, square = carry
        for pr in range(2):
            row = 2 * r + pr
            strip = row // SR
            within = row - strip * SR
            for image in range(2):
                spot = pr * 2 + image
                line_tmp[spot, 0:CW] = strips[image * STRIPS + strip, within].astype(f32)
                for pc in range(2):
                    x_ref[pr * 2 + pc, r, pl.ds(image, W3, stride=2)] = line_tmp[
                        spot, pl.ds(pc, W3, stride=2)
                    ]
            for pc in range(2):
                plane = pr * 2 + pc
                valid = row < reach[pc]
                inv_ref[plane, r] = jnp.where(
                    valid, line(row_share(row, high)) * col_share[pc], 0.0
                )
                values = jnp.where(valid, x_ref[plane, r], 0.0)
                x_ref[plane, r] = values
                total = total + fold(values)
                square = square + fold(values * values)
        inv3_ref[r] = jnp.where(r < reach3, line(row_share(r, high3)) * col_share3, 0.0)
        return (total, square)

    nothing = jnp.zeros((8, C2), f32)
    nothing3 = jnp.zeros((8, WIDE), f32)
    total, square = lax.fori_loop(0, H3, arrange, (nothing, nothing))
    mean1, scaling1 = norm_terms(total, square, count_two)
    factor1 = line(scaling1 * gain1)
    shift1 = line(bias1 - mean1 * scaling1 * gain1)

    def window_cols(k, carry):
        rows = pl.ds(2 * k, 2)
        for pr in range(2):
            masked = []
            for pc in range(2):
                plane = pr * 2 + pc
                normal = rounded(x_ref[plane, rows] * factor1 + shift1)
                masked.append(jnp.where(inv_ref[plane, rows] > 0.0, normal, 0.0))
            both = masked[0] + masked[1]
            col_ref[pr * 2, pl.ds(2 * k + 1, 2)] = both + from_left(masked[1])
            col_ref[pr * 2 + 1, pl.ds(2 * k + 1, 2)] = both + from_right(masked[0])
        return carry

    lax.fori_loop(0, H3 // 2, window_cols, 0)

    def row_windows(pc, k):
        even = col_ref[pc, pl.ds(2 * k + 1, 2)]
        odd = col_ref[2 + pc, pl.ds(2 * k + 1, 2)]
        both = even + odd
        return (both + col_ref[2 + pc, pl.ds(2 * k, 2)], both + col_ref[pc, pl.ds(2 * k + 2, 2)])

    def mix(k, carry):
        total, square = carry
        rows = pl.ds(2 * k, 2)
        for pc in range(2):
            windows = row_windows(pc, k)
            for pr in range(2):
                plane = pr * 2 + pc
                values = x_ref[plane, rows]
                share = inv_ref[plane, rows]
                pooled = windows[pr] * share - rounded(values * factor1 + shift1)
                pooled = jnp.where(share > 0.0, pooled, 0.0)
                mixed = values + scale1 * pooled
                pool_ref[plane, rows] = pooled
                mix_ref[plane, rows] = mixed
                total = total + fold(mixed)
                square = square + fold(mixed * mixed)
        return (total, square)

    total, square = lax.fori_loop(0, H3 // 2, mix, (nothing, nothing))
    mean2, scaling2 = norm_terms(total, square, count_two)
    factor2 = line(scaling2 * gain2)
    shift2 = line(bias2 - mean2 * scaling2 * gain2)

    def where_chunk(c):
        plane = c // STEPS
        first = (c - plane * STEPS) * ROWS
        return (plane, first, pl.ds(pl.multiple_of(c * CHUNK, CHUNK), CHUNK))

    def branch(c, carry):
        plane, first, flat = where_chunk(c)
        mixed = mix_ref[plane, pl.ds(first, ROWS)]
        low = (mixed * factor2 + shift2).reshape(CHUNK, C2).astype(bf16)
        h_ref[flat] = low
        hidden = product(low, w1_ref[...]) + vec_hid_two_ref[...]
        active, slope = gelu_pair(hidden)
        active = active.astype(bf16)
        u_ref[flat] = active
        g_ref[flat] = slope.astype(bf16)
        out = (product(active, w2_ref[...]) + out_bias).reshape(ROWS, LINE, C2)
        valid = inv_ref[plane, pl.ds(first, ROWS)] > 0.0
        zed = rounded(jnp.where(valid, mixed + scale2 * out, 0.0))
        zed_ref[plane, pl.ds(first + 1, ROWS)] = zed
        return carry

    lax.fori_loop(0, 4 * STEPS, branch, 0)

    def patches(k, carry):
        flat = pl.ds(pl.multiple_of(k * 2 * LINE, 2 * LINE), 2 * LINE)
        for ky in range(3):
            pr = (0 if ky == 1 else 1) * 2
            rows = pl.ds(2 * k + (0 if ky == 0 else 1), 2)
            even = zed_ref[pr, rows]
            odd = zed_ref[pr + 1, rows]
            for kx, tap in enumerate((from_left(odd), even, odd)):
                at = (3 * ky + kx) * C2
                patch_ref[flat, at : at + C2] = tap.reshape(2 * LINE, C2).astype(bf16)
        return carry

    lax.fori_loop(0, H3 // 2, patches, 0)

    def embed(c, carry):
        total, square = carry
        flat = pl.ds(pl.multiple_of(c * CHUNK, CHUNK), CHUNK)
        rows = pl.ds(c * ROWS, ROWS)
        out = (product(patch_ref[flat], we_ref[...]) + embed_bias).reshape(ROWS, LINE, WIDE)
        out = jnp.where(widen(inv3_ref[rows]) > 0.0, out, 0.0)
        e_ref[rows] = out
        return (total + fold(out), square + fold(out * out))

    total, square = lax.fori_loop(0, STEPS, embed, (nothing3, nothing3))
    mean3, scaling3 = norm_terms(total, square, count_three)
    factor3 = line(scaling3 * gain3)
    shift3 = line(bias3 - mean3 * scaling3 * gain3)

    def window_cols3(k, carry):
        rows = pl.ds(2 * k, 2)
        normal = rounded(e_ref[rows] * factor3 + shift3)
        masked = jnp.where(widen(inv3_ref[rows]) > 0.0, normal, 0.0)
        col3_ref[pl.ds(2 * k + 1, 2)] = masked + from_left(masked) + from_right(masked)
        return carry

    lax.fori_loop(0, H3 // 2, window_cols3, 0)

    def row_windows3(k):
        return (
            col3_ref[pl.ds(2 * k, 2)]
            + col3_ref[pl.ds(2 * k + 1, 2)]
            + col3_ref[pl.ds(2 * k + 2, 2)]
        )

    def mix3(k, carry):
        total, square = carry
        rows = pl.ds(2 * k, 2)
        values = e_ref[rows]
        share = widen(inv3_ref[rows])
        pooled = row_windows3(k) * share - rounded(values * factor3 + shift3)
        pooled = jnp.where(share > 0.0, pooled, 0.0)
        mixed = values + scale3 * pooled
        pool3_ref[rows] = pooled
        mix3_ref[rows] = mixed
        return (total + fold(mixed), square + fold(mixed * mixed))

    total, square = lax.fori_loop(0, H3 // 2, mix3, (nothing3, nothing3))
    mean4, scaling4 = norm_terms(total, square, count_three)
    factor4 = line(scaling4 * gain4)
    shift4 = line(bias4 - mean4 * scaling4 * gain4)
    normal4 = (spread(scaling4, WIDE), spread(-mean4 * scaling4, WIDE))

    def branch3(c, carry):
        d_out_bias, d_scale, d_hidden_bias, d_shift, d_gain = carry
        flat = pl.ds(pl.multiple_of(c * CHUNK, CHUNK), CHUNK)
        rows = pl.ds(c * ROWS, ROWS)
        mixed = mix3_ref[rows]
        low = (mixed * factor4 + shift4).reshape(CHUNK, WIDE).astype(bf16)
        h3_ref[flat] = low
        hidden = product(low, w3_ref[...]) + vec_hid_three_ref[...]
        active, slope = gelu_pair(hidden)
        active = active.astype(bf16)
        u3_ref[flat] = active
        out = (product(active, w4_ref[...]) + out_bias3).reshape(ROWS, LINE, WIDE)
        valid = widen(inv3_ref[rows]) > 0.0
        out = jnp.where(valid, out, 0.0)
        result_ref[0, rows] = mixed + scale4 * out
        goal = jnp.where(valid, goal_ref[0, flat].astype(f32).reshape(ROWS, LINE, WIDE), 0.0)
        low_goal = (scale4 * goal).reshape(CHUNK, WIDE).astype(bf16)
        dy3_ref[flat] = low_goal
        d_hidden = (slope * product_nt(low_goal, w4_ref[...])).astype(bf16)
        g3_ref[flat] = d_hidden
        d_low = product_nt(d_hidden, w3_ref[...]).reshape(ROWS, LINE, WIDE)
        dx3_ref[rows] = d_low
        normal = mixed * normal4[0] + normal4[1]
        return (
            d_out_bias + fold(low_goal.astype(f32)),
            d_scale + fold(out * goal),
            d_hidden_bias + fold(d_hidden.astype(f32)),
            d_shift + fold(d_low),
            d_gain + fold(d_low * normal),
        )

    wide_zero = jnp.zeros((8, HID3), f32)
    d_out_bias, d_scale, d_hidden_bias, d_shift, d_gain = lax.fori_loop(
        0, STEPS, branch3, (nothing3, nothing3, wide_zero, nothing3, nothing3)
    )
    acc_three[7] += d_out_bias
    acc_three[6] += d_scale
    acc_hid_three[...] += d_hidden_bias
    acc_three[5] += d_shift
    acc_three[4] += d_gain
    mean_shift = by_image(d_shift * gain4) / count_three
    mean_gain = by_image(d_gain * gain4) / count_three

    def keep(ref, value):
        if pairs == 1:
            ref[...] = value
        else:

            @pl.when(pair == 0)
            def _():
                ref[...] = value

            @pl.when(pair > 0)
            def _():
                ref[...] += value

    keep(gw3_ref, product_tn(h3_ref[...], g3_ref[...]))
    keep(gw4_ref, product_tn(u3_ref[...], dy3_ref[...]))

    back_gain4 = line(scaling4 * gain4)
    back_mean4 = spread(scaling4 * mean_shift, WIDE)
    back_normal4 = spread(scaling4 * mean_gain, WIDE)

    def unmix3(k, d_scale):
        rows = pl.ds(2 * k, 2)
        flat = pl.ds(pl.multiple_of(k * 2 * LINE, 2 * LINE), 2 * LINE)
        share = widen(inv3_ref[rows])
        valid = share > 0.0
        normal = mix3_ref[rows] * normal4[0] + normal4[1]
        back = dx3_ref[rows] * back_gain4 - back_mean4 - normal * back_normal4
        goal = goal_ref[0, flat].astype(f32).reshape(2, LINE, WIDE)
        d_mixed = jnp.where(valid, back + goal, 0.0)
        dx3_ref[rows] = d_mixed
        d_scale = d_scale + fold(pool3_ref[rows] * d_mixed)
        weighted = scale3 * d_mixed * share
        col3_ref[pl.ds(2 * k + 1, 2)] = weighted + from_left(weighted) + from_right(weighted)
        return d_scale

    acc_three[3] += lax.fori_loop(0, H3 // 2, unmix3, nothing3)
    normal3 = (spread(scaling3, WIDE), spread(-mean3 * scaling3, WIDE))

    def unpool3(k, carry):
        d_shift, d_gain = carry
        rows = pl.ds(2 * k, 2)
        valid = widen(inv3_ref[rows]) > 0.0
        d_normal = jnp.where(valid, row_windows3(k) - scale3 * dx3_ref[rows], 0.0)
        pool3_ref[rows] = d_normal
        normal = e_ref[rows] * normal3[0] + normal3[1]
        return (d_shift + fold(d_normal), d_gain + fold(d_normal * normal))

    d_shift, d_gain = lax.fori_loop(0, H3 // 2, unpool3, (nothing3, nothing3))
    acc_three[2] += d_shift
    acc_three[1] += d_gain
    mean_shift = by_image(d_shift * gain3) / count_three
    mean_gain = by_image(d_gain * gain3) / count_three
    back_gain3 = line(scaling3 * gain3)
    back_mean3 = spread(scaling3 * mean_shift, WIDE)
    back_normal3 = spread(scaling3 * mean_gain, WIDE)

    def unnorm3(k, d_bias):
        rows = pl.ds(2 * k, 2)
        flat = pl.ds(pl.multiple_of(k * 2 * LINE, 2 * LINE), 2 * LINE)
        valid = widen(inv3_ref[rows]) > 0.0
        normal = e_ref[rows] * normal3[0] + normal3[1]
        back = pool3_ref[rows] * back_gain3 - back_mean3 - normal * back_normal3
        low = jnp.where(valid, dx3_ref[rows] + back, 0.0).astype(bf16)
        dpre_ref[flat] = low.reshape(2 * LINE, WIDE)
        return d_bias + fold(low.astype(f32))

    acc_three[0] += lax.fori_loop(0, H3 // 2, unnorm3, nothing3)
    keep(gwe_ref, product_tn(patch_ref[...], dpre_ref[...]))

    def unpatch(c, carry):
        flat = pl.ds(pl.multiple_of(c * CHUNK, CHUNK), CHUNK)
        rows = pl.ds(c * ROWS, ROWS)
        dpatch_ref[rows] = product_nt(dpre_ref[flat], we_ref[...]).reshape(ROWS, LINE, 9 * C2)
        return carry

    lax.fori_loop(0, STEPS, unpatch, 0)
    dpatch_ref[H3 : H3 + 1] = jnp.zeros((1, LINE, 9 * C2), f32)

    def tap(ky, kx, rows):
        at = (3 * ky + kx) * C2
        return dpatch_ref[rows, :, at : at + C2]

    def gather_back(k, carry):
        here = pl.ds(2 * k, 2)
        below = pl.ds(2 * k + 1, 2)
        sources = []
        for ky, rows in ((0, below), (1, here), (2, here)):
            sources.append((tap(ky, 1, rows), tap(ky, 2, rows) + from_right(tap(ky, 0, rows))))
        for pc in range(2):
            for pr, value in ((0, sources[1][pc]), (1, sources[2][pc] + sources[0][pc])):
                plane = pr * 2 + pc
                valid = inv_ref[plane, here] > 0.0
                zed_ref[plane, here] = jnp.where(valid, rounded(value), 0.0)
        return carry

    lax.fori_loop(0, H3 // 2, gather_back, 0)

    normal2 = (spread(scaling2, C2), spread(-mean2 * scaling2, C2))

    def unbranch(c, carry):
        d_out_bias, d_hidden_bias, d_shift, d_gain = carry
        plane, first, flat = where_chunk(c)
        rows = pl.ds(first, ROWS)
        low_goal = (scale2 * zed_ref[plane, rows]).reshape(CHUNK, C2).astype(bf16)
        dy_ref[flat] = low_goal
        d_hidden = g_ref[flat].astype(f32) * product_nt(low_goal, w2_ref[...])
        d_hidden = d_hidden.astype(bf16)
        g_ref[flat] = d_hidden
        d_low = product_nt(d_hidden, w1_ref[...]).reshape(ROWS, LINE, C2)
        dx_ref[plane, rows] = d_low
        normal = mix_ref[plane, rows] * normal2[0] + normal2[1]
        return (
            d_out_bias + fold(low_goal.astype(f32)),
            d_hidden_bias + fold(d_hidden.astype(f32)),
            d_shift + fold(d_low),
            d_gain + fold(d_low * normal),
        )

    d_out_bias, d_hidden_bias, d_shift, d_gain = lax.fori_loop(
        0, 4 * STEPS, unbranch, (nothing, jnp.zeros((8, HID2), f32), nothing, nothing)
    )
    acc_two[6] += d_out_bias
    acc_hid_two[...] += d_hidden_bias
    acc_two[4] += d_shift
    acc_two[3] += d_gain
    mean_shift = by_image(d_shift * gain2) / count_two
    mean_gain = by_image(d_gain * gain2) / count_two
    keep(gw1_ref, product_tn(h_ref[...], g_ref[...]))
    new_gw2 = product_tn(dy_ref[...], u_ref[...]).T
    keep(gw2_ref, new_gw2)
    d_scale = fold(w2_ref[...].astype(f32) * new_gw2) + out_bias * d_out_bias
    acc_two[5] += d_scale / scale2

    back_gain2 = line(scaling2 * gain2)
    back_mean2 = spread(scaling2 * mean_shift, C2)
    back_normal2 = spread(scaling2 * mean_gain, C2)

    def unmix(k, d_scale):
        rows = pl.ds(2 * k, 2)
        for pr in range(2):
            weighted = []
            for pc in range(2):
                plane = pr * 2 + pc
                share = inv_ref[plane, rows]
                normal = mix_ref[plane, rows] * normal2[0] + normal2[1]
                back = dx_ref[plane, rows] * back_gain2 - back_mean2 - normal * back_normal2
                d_mixed = jnp.where(share > 0.0, zed_ref[plane, rows] + back, 0.0)
                dx_ref[plane, rows] = d_mixed
                d_scale = d_scale + fold(pool_ref[plane, rows] * d_mixed)
                weighted.append(scale1 * d_mixed * share)
            both = weighted[0] + weighted[1]
            col_ref[pr * 2, pl.ds(2 * k + 1, 2)] = both + from_left(weighted[1])
            col_ref[pr * 2 + 1, pl.ds(2 * k + 1, 2)] = both + from_right(weighted[0])
        return d_scale

    acc_two[2] += lax.fori_loop(0, H3 // 2, unmix, nothing)
    normal1 = (spread(scaling1, C2), spread(-mean1 * scaling1, C2))

    def unpool(k, carry):
        d_shift, d_gain = carry
        rows = pl.ds(2 * k, 2)
        for pc in range(2):
            windows = row_windows(pc, k)
            for pr in range(2):
                plane = pr * 2 + pc
                valid = inv_ref[plane, rows] > 0.0
                d_normal = windows[pr] - scale1 * dx_ref[plane, rows]
                d_normal = jnp.where(valid, d_normal, 0.0)
                pool_ref[plane, rows] = d_normal
                normal = x_ref[plane, rows] * normal1[0] + normal1[1]
                d_shift = d_shift + fold(d_normal)
                d_gain = d_gain + fold(d_normal * normal)
        return (d_shift, d_gain)

    d_shift, d_gain = lax.fori_loop(0, H3 // 2, unpool, (nothing, nothing))
    acc_two[1] += d_shift
    acc_two[0] += d_gain
    mean_shift = by_image(d_shift * gain1) / count_two
    mean_gain = by_image(d_gain * gain1) / count_two
    back_gain1 = line(scaling1 * gain1)
    back_mean1 = spread(scaling1 * mean_shift, C2)
    back_normal1 = spread(scaling1 * mean_gain, C2)

    def unnorm(r, carry):
        for pr in range(2):
            row = 2 * r + pr
            strip = row // SR
            within = row - strip * SR
            for pc in range(2):
                plane = pr * 2 + pc
                normal = x_ref[plane, r] * normal1[0] + normal1[1]
                back = pool_ref[plane, r] * back_gain1 - back_mean1 - normal * back_normal1
                dx_ref[plane, r] = jnp.where(
                    inv_ref[plane, r] > 0.0, dx_ref[plane, r] + back, 0.0
                )
            for image in range(2):
                spot = pr * 2 + image
                for pc in range(2):
                    line_tmp[spot, pl.ds(pc, W3, stride=2)] = dx_ref[
                        pr * 2 + pc, r, pl.ds(image, W3, stride=2)
                    ]
                strips[image * STRIPS + strip, within] = line_tmp[spot, 0:CW].astype(bf16)
        return carry

    lax.fori_loop(0, H3, unnorm, 0)
    for copy in strip_copies(True):
        copy.start()

    @pl.when(pair == pairs - 1)
    def _():
        offset = 0
        for (rows, cols), ref in zip(SHAPES, grads):
            wide = cols // BS
            for rb in range(rows // BS):
                for cb in range(0, wide, 2):
                    number = offset + rb * wide + cb
                    at = slice(cb * BS, cb * BS + 128)
                    top = ref[rb * BS : rb * BS + HALF, at]
                    low = ref[rb * BS + HALF : rb * BS + BS, at]
                    grad_ref[place_ref[number]] = jnp.where(
                        left_half, top, pltpu.roll(low, BS, 1)
                    ).astype(bf16)
                    if cb + 1 < wide:
                        grad_ref[place_ref[number + 1]] = jnp.where(
                            left_half, pltpu.roll(top, BS, 1), low
                        ).astype(bf16)
            offset += rows // BS * wide

        def filler(number, carry):
            grad_ref[place_ref[number]] = jnp.zeros((HALF, 128), bf16)
            return carry

        lax.fori_loop(USED, slots, filler, 0)

        flat_ref[...] = jnp.zeros(flat_ref.shape, f32)

        def put(at, total, length):
            if at % 128:
                room = jnp.zeros((8, 128), f32)
                if total.shape[1] < length + BS:
                    total = jnp.concatenate([total, room], axis=1)
                total = pltpu.roll(total, BS, 1)
            whole = jnp.sum(total, axis=0, keepdims=True)
            done = -(at % 128)
            row = at // 128
            lane = 0
            while done < length:
                first = max(0, -done)
                last = min(128, length - done)
                flat_ref[row : row + 1, first:last] = whole[:, lane + first : lane + last]
                done += 128
                lane += 128
                row += 1

        at = 0
        for n in range(6):
            put(at, acc_two[n], C2)
            at += C2
        put(at, acc_hid_two[...], HID2)
        at += HID2
        put(at, acc_two[6], C2)
        at += C2
        for n in range(7):
            put(at, acc_three[n], C3)
            at += C3
        put(at, acc_hid_three[...], HID3)
        at += HID3
        put(at, acc_three[7], C3)
        packed = flat_ref[...].astype(bf16)
        stride = slots // strip_count + extra
        for n in range(extra):
            piece = packed[n * HALF : (n + 1) * HALF]

            def leave(target, carry):
                grad_ref[target * stride + stride - extra + n] = piece
                return carry

            lax.fori_loop(0, strip_count, leave, 0)

    for copy in strip_copies(True):
        copy.wait()


def run_main(slot_of, place_of, sizes, strips, goal, gathered, vec_two, vec_hid_two, vec_three, vec_hid_three, extra):
    strip_count = strips.shape[0]
    pairs = goal.shape[0]
    slots = gathered.shape[0]
    rows_out = slots + extra * strip_count

    def whole(shape):
        return pl.BlockSpec(shape, lambda t: (0,) * len(shape), pipeline_mode=pl.Buffered(1))

    smem = pl.BlockSpec(memory_space=pltpu.SMEM)
    anywhere = pl.BlockSpec(memory_space=pl.ANY)
    plane_f32 = pltpu.VMEM((4, H3, LINE, C2), f32)
    wide_f32 = pltpu.VMEM((H3, LINE, WIDE), f32)
    scratch = [
        pltpu.VMEM((2 * STRIPS, SR, CW, C2), bf16),
        pltpu.VMEM((4, LINE, C2), f32),
        plane_f32,
        plane_f32,
        pltpu.VMEM((4, H3 + 2, LINE, C2), f32),
        plane_f32,
        plane_f32,
        pltpu.VMEM((4, H3 + 1, LINE, C2), f32),
        plane_f32,
        pltpu.VMEM((4 * PLANE, HID2), bf16),
        pltpu.VMEM((4 * PLANE, HID2), bf16),
        pltpu.VMEM((4 * PLANE, C2), bf16),
        pltpu.VMEM((4 * PLANE, C2), bf16),
        pltpu.VMEM((PLANE, 9 * C2), bf16),
        pltpu.VMEM((H3 + 1, LINE, 9 * C2), f32),
        pltpu.VMEM((H3, LINE, 128), f32),
        wide_f32,
        pltpu.VMEM((H3 + 2, LINE, WIDE), f32),
        wide_f32,
        wide_f32,
        wide_f32,
        pltpu.VMEM((PLANE, HID3), bf16),
        pltpu.VMEM((PLANE, HID3), bf16),
        pltpu.VMEM((PLANE, WIDE), bf16),
        pltpu.VMEM((PLANE, WIDE), bf16),
        pltpu.VMEM((PLANE, WIDE), bf16),
        pltpu.VMEM((C2, HID2), bf16),
        pltpu.VMEM((HID2, C2), bf16),
        pltpu.VMEM((9 * C2, WIDE), bf16),
        pltpu.VMEM((WIDE, HID3), bf16),
        pltpu.VMEM((HID3, WIDE), bf16),
        pltpu.VMEM((C2, HID2), f32),
        pltpu.VMEM((HID2, C2), f32),
        pltpu.VMEM((9 * C2, WIDE), f32),
        pltpu.VMEM((WIDE, HID3), f32),
        pltpu.VMEM((HID3, WIDE), f32),
        pltpu.VMEM((7, 8, C2), f32),
        pltpu.VMEM((8, HID2), f32),
        pltpu.VMEM((8, 8, WIDE), f32),
        pltpu.VMEM((8, HID3), f32),
        pltpu.VMEM((extra * HALF, 128), f32),
        pltpu.SemaphoreType.DMA((4,)),
        pltpu.SemaphoreType.DMA((4,)),
    ]
    return pl.pallas_call(
        functools.partial(main_kernel, pairs, strip_count, slots, extra),
        grid=(pairs,),
        in_specs=[
            smem,
            smem,
            smem,
            anywhere,
            pl.BlockSpec((1,) + goal.shape[1:], lambda t: (t, 0, 0)),
            whole(gathered.shape),
            whole(vec_two.shape),
            whole(vec_hid_two.shape),
            whole(vec_three.shape),
            whole(vec_hid_three.shape),
        ],
        out_specs=[
            pl.BlockSpec((1, H3, LINE, WIDE), lambda t: (t, 0, 0, 0)),
            anywhere,
            whole((rows_out, HALF, 128)),
        ],
        out_shape=[
            jax.ShapeDtypeStruct((pairs, H3, LINE, WIDE), f32),
            jax.ShapeDtypeStruct(strips.shape, bf16),
            jax.ShapeDtypeStruct((rows_out, HALF, 128), bf16),
        ],
        scratch_shapes=scratch,
        compiler_params=pltpu.CompilerParams(vmem_limit_bytes=62 * 1024 * 1024),
        name="blocks",
    )(slot_of, place_of, sizes, strips, goal, gathered, vec_two, vec_hid_two, vec_three, vec_hid_three)


def pack_kernel(master_ref, dense_ref):
    values = master_ref[...]
    dense_ref[...] = jnp.concatenate([values[:, :HALF], values[:, HALF:]], axis=2).astype(bf16)


def pack(master):
    owned = master.shape[0]
    return pl.pallas_call(
        pack_kernel,
        out_shape=jax.ShapeDtypeStruct((owned, HALF, 2 * BS), bf16),
        name="pack",
    )(master)


def fold_tile_kernel(spot_ref, pieces_ref, own_ref, *part_refs):
    groups = len(part_refs) + 1
    share = own_ref.shape[0]
    for k in range(groups):
        start = lax.rem(spot_ref[0] + k, groups) * share
        total = pieces_ref[0, pl.ds(start, share)].astype(f32)
        for n in range(1, pieces_ref.shape[0]):
            total = total + pieces_ref[n, pl.ds(start, share)].astype(f32)
        if k == 0:
            own_ref[...] = total
        else:
            part_refs[k - 1][...] = total.astype(bf16)


def fold_tile(spot, pieces, groups):
    share = pieces.shape[1] // groups
    part = jax.ShapeDtypeStruct((share,) + pieces.shape[2:], bf16)
    own = jax.ShapeDtypeStruct(part.shape, f32)
    return pl.pallas_call(
        fold_tile_kernel,
        in_specs=[pl.BlockSpec(memory_space=pltpu.SMEM), pl.BlockSpec(memory_space=pltpu.VMEM)],
        out_shape=[own] + [part] * (groups - 1),
        name="fold_tile",
    )(spot, pieces)


def fold_batch_kernel(owned, vector_weight, spot_ref, own_ref, *refs):
    part_refs, (total_ref, norm_ref) = refs[:-2], refs[-2:]
    share = own_ref.shape[0]
    square = jnp.zeros((8, 128), f32)
    for n in range(share):
        total = own_ref[n]
        for ref in part_refs:
            total = total + ref[n].astype(f32)
        total_ref[n] = total.astype(bf16)
        weight = jnp.where(spot_ref[0] * share + n < owned, 1.0, vector_weight)
        square = square + weight * fold(total * total)
    square = jnp.sum(jnp.sum(square, axis=1, keepdims=True), axis=0, keepdims=True)
    norm_ref[...] = jnp.broadcast_to(square[None], norm_ref.shape)


def fold_batch(spot, own, parts, owned, tile_count):
    count = tile_count * (len(parts) + 1)
    vmem = pl.BlockSpec(memory_space=pltpu.VMEM)
    return pl.pallas_call(
        functools.partial(fold_batch_kernel, owned, 1.0 / tile_count),
        in_specs=[pl.BlockSpec(memory_space=pltpu.SMEM)] + [vmem] * (len(parts) + 1),
        out_shape=[
            jax.ShapeDtypeStruct(own.shape, bf16),
            jax.ShapeDtypeStruct((count, 1, 128), f32),
        ],
        name="fold_batch",
    )(spot, own, *parts)


def update_kernel(owned, groups, spot_ref, norm_ref, *refs):
    quarters = refs[:groups]
    (
        master_ref,
        left_stat_ref,
        right_stat_ref,
        left_root_ref,
        right_root_ref,
        grad_ref,
        left_ref,
        right_ref,
        new_ref,
        copy_ref,
        vector_ref,
        clip_ref,
    ) = refs[groups:]
    share = quarters[0].shape[0]
    part = grad_ref.shape[0]
    step = pl.program_id(0)
    norm = jnp.sqrt(jnp.sum(norm_ref[...], axis=0))
    factor = jnp.minimum(1.0, clip_limit / norm)

    def summed(number):
        source = number // share
        local = number - source * share
        turn = lax.rem(spot_ref[0] - source + groups, groups)
        value = quarters[0][local].astype(f32)
        for k in range(1, groups):
            value = jnp.where(turn == k, quarters[k][local].astype(f32), value)
        return value * factor

    @pl.when(step == 0)
    def _():
        clip_ref[...] = norm
        for n in range(vector_ref.shape[0]):
            vector_ref[n] = summed(owned + n)

    for n in range(part):
        dense = summed(jnp.minimum(step * part + n, owned - 1))
        grad = jnp.concatenate([dense[:, :BS], dense[:, BS:]], axis=0)
        grad_ref[n] = grad
        low = grad.astype(bf16)
        left_ref[n] = 0.5 * left_stat_ref[n] + 0.5 * product_nt(low, low)
        right_ref[n] = 0.5 * right_stat_ref[n] + 0.5 * product_tn(low, low)
        stepped = product(left_root_ref[n].astype(bf16), low).astype(bf16)
        stepped = product(stepped, right_root_ref[n].astype(bf16))
        new = master_ref[n] - rate_matrix * stepped
        new_ref[n] = new
        copy_ref[n] = new.astype(bf16)


def update(spot, norm, quarters, extra, master, *stats):
    owned = master.shape[0]
    part = min(owned, 7)
    groups = len(quarters)
    square = pl.BlockSpec((part, BS, BS), lambda t: (t, 0, 0))
    shape = jax.ShapeDtypeStruct(master.shape, f32)

    def whole(shape):
        return pl.BlockSpec(shape, lambda t: (0,) * len(shape))

    return pl.pallas_call(
        functools.partial(update_kernel, owned, groups),
        grid=(-(-owned // part),),
        in_specs=[pl.BlockSpec(memory_space=pltpu.SMEM), whole(norm.shape)]
        + [whole(quarters[0].shape)] * groups
        + [square] * 5,
        out_specs=[square] * 5 + [whole((extra, HALF, 128)), whole((1, 128))],
        out_shape=[shape] * 4
        + [
            jax.ShapeDtypeStruct(master.shape, bf16),
            jax.ShapeDtypeStruct((extra, HALF, 128), f32),
            jax.ShapeDtypeStruct((1, 128), f32),
        ],
        compiler_params=pltpu.CompilerParams(vmem_limit_bytes=32 * 1024 * 1024),
        name="update",
    )(spot, norm, *quarters, master, *stats)


def share_out(pieces, axis):
    return lax.all_to_all(pieces, axis, split_axis=0, concat_axis=0, tiled=True)


def on_device(
    pixels,
    buckets,
    slot_owner_table,
    out_grad,
    master,
    left_stat,
    right_stat,
    left_root,
    right_root,
    vectors,
    moment,
):
    tile_count = lax.axis_size("tile")
    tile_place = lax.axis_index("tile")
    slot_count = pixels.shape[2]
    group_count = tile_count // STRIPS
    pairs = group_count // 2
    owned = master.shape[0]
    slots = owned * tile_count
    batch_count = lax.axis_size("batch")
    spot = lax.axis_index("batch").astype(jnp.int32).reshape(1)
    extra = extra_of(owned, batch_count)
    strips = share_out(pixels.reshape((tile_count,) + pixels.shape[3:]), "tile")
    gathered = lax.all_gather(pack(master), "tile", axis=0, tiled=True)

    numbers = jnp.arange(slots, dtype=jnp.int32)
    slot_of = jnp.sum(
        jnp.where(slot_owner_table[None, :] == numbers[:, None], numbers[None, :], 0), axis=1
    )
    place_of = slot_of + extra * (slot_of // owned)
    image_ids = lax.dynamic_index_in_dim(
        buckets.reshape(group_count, slot_count), tile_place, 1, keepdims=False
    )
    heights = jnp.where(image_ids == 0, 5 * CH // 9, jnp.where(image_ids == 1, 7 * CH // 9, CH))
    breadths = jnp.where(image_ids == 0, CW, jnp.where(image_ids == 1, 7 * CW // 9, 5 * CW // 9))
    sizes = jnp.stack([heights, breadths], axis=1).reshape(-1).astype(jnp.int32)

    two = 6 * C2 + HID2 + C2
    vec_two = jnp.concatenate([vectors[: 6 * C2], vectors[6 * C2 + HID2 : two]]).reshape(7, C2)
    vec_hid_two = vectors[6 * C2 : 6 * C2 + HID2].reshape(1, HID2)
    wide_end = two + 7 * C3
    vec_three = jnp.concatenate([vectors[two:wide_end], vectors[wide_end + HID3 :]])
    vec_three = jnp.pad(vec_three.reshape(8, C3), ((0, 0), (0, WIDE - C3)))
    vec_hid_three = vectors[wide_end : wide_end + HID3].reshape(1, HID3)

    goal = out_grad.reshape(pairs, 2, H3, W3, C3).transpose(0, 2, 3, 1, 4)
    goal = goal.reshape(pairs, H3, 2 * W3, C3)
    goal = jnp.pad(goal, ((0, 0), (0, 0), (0, LINE - 2 * W3), (0, WIDE - C3)))
    goal = goal.reshape(pairs, PLANE, WIDE)

    result, pixel_back, outgoing = run_main(
        slot_of,
        place_of,
        sizes,
        strips,
        goal,
        gathered,
        vec_two,
        vec_hid_two,
        vec_three,
        vec_hid_three,
        extra,
    )
    result = result[:, :, : 2 * W3, :C3].reshape(pairs, H3, W3, 2, C3).transpose(0, 3, 1, 2, 4)

    outgoing = outgoing.reshape(tile_count, owned + extra, HALF, 128)
    arrived = share_out(outgoing, "tile")
    own, *parts = fold_tile(spot, arrived, batch_count)
    parts = [
        lax.ppermute(part, "batch", [(i, (i + k + 1) % batch_count) for i in range(batch_count)])
        for k, part in enumerate(parts)
    ]
    quarter, norm = fold_batch(spot, own, parts, owned, tile_count)
    quarters = [quarter] + [
        lax.ppermute(quarter, "batch", [(i, (i + k) % batch_count) for i in range(batch_count)])
        for k in range(1, batch_count)
    ]
    norm = share_out(norm, ("batch", "tile"))
    block_grad, left_new, right_new, master_new, weight_copy, whole_vector, clip = update(
        spot, norm, quarters, extra, master, left_stat, right_stat, left_root, right_root
    )
    clip_norm = clip[0, 0]
    share = vectors.shape[0] // tile_count
    whole_vector = whole_vector.reshape(-1)
    vec_grad = lax.dynamic_slice_in_dim(whole_vector, tile_place * share, share, 0)
    vec_moment = moment + vec_grad * vec_grad
    own_vectors = lax.dynamic_slice_in_dim(vectors, tile_place * share, share, 0)
    vec_new = own_vectors - rate_vector * vec_grad / (jnp.sqrt(vec_moment) + eps_adagrad)
    returned = share_out(pixel_back, "tile")
    return (
        result.reshape(out_grad.shape),
        returned.astype(f32).reshape(pixels.shape),
        clip_norm,
        block_grad,
        left_new,
        right_new,
        master_new,
        weight_copy,
        vec_grad,
        vec_moment,
        vec_new,
    )


def solution(mesh):
    placed = (
        P("batch", "tile", None, None, None, None),
        P("batch"),
        P(),
        P("batch", "tile", None, None, None, None, None),
        P("tile", None, None),
        P("tile", None, None),
        P("tile", None, None),
        P("tile", None, None),
        P("tile", None, None),
        P(),
        P("tile"),
    )
    return jax.shard_map(
        on_device,
        mesh=mesh,
        in_specs=placed,
        out_specs=(
            P("batch", "tile", None, None, None, None, None),
            P("batch", "tile", None, None, None, None),
            P(),
            P("tile", None, None),
            P("tile", None, None),
            P("tile", None, None),
            P("tile", None, None),
            P("tile", None, None),
            P("tile"),
            P("tile"),
            P("tile"),
        ),
        check_vma=False,
    )
```

```python
import functools

import jax
import jax.numpy as jnp
from jax import lax
from jax.experimental import pallas as pl
from jax.experimental.pallas import tpu as pltpu
from jax.sharding import PartitionSpec as P

C2 = 128
HID2 = 512
C3 = 320
HID3 = 1280
CH = 36
CW = 36
STRIPS = 4
BS = 64
SR = CH // STRIPS
H3 = CH // 2
W3 = CW // 2
WIDE = 384
LINE = 40
PLANE = H3 * LINE
ROWS = 6
CHUNK = ROWS * LINE
STEPS = H3 // ROWS
HALF = BS // 2

eps_norm = 1e-05
clip_limit = 1.0
rate_matrix = 0.3
rate_vector = 0.3
eps_adagrad = 1e-08
f32 = jnp.float32
bf16 = jnp.bfloat16

SHAPES = [(C2, HID2), (HID2, C2), (9 * C2, C3), (C3, HID3), (HID3, C3)]
USED = sum(rows // BS * (cols // BS) for rows, cols in SHAPES)
VEC_ROWS = (6 * C2 + HID2 + C2 + C3 + 6 * C3 + HID3 + C3) // 128


def extra_of(owned, groups):
    extra = -(-VEC_ROWS // HALF)
    return extra + -(owned + extra) % groups


def product(left, right):
    return jnp.dot(left, right, preferred_element_type=f32)


def product_nt(left, right):
    return lax.dot_general(left, right, (((1,), (1,)), ((), ())), preferred_element_type=f32)


def product_tn(left, right):
    return lax.dot_general(left, right, (((0,), (0,)), ((), ())), preferred_element_type=f32)


def gelu_pair(values):
    bell = jnp.exp2(values * values * (-0.5 * 1.4426950408889634))
    step = pl.reciprocal(1.0 + (0.3275911 * 0.7071067811865476) * jnp.abs(values), approx=True)
    tail = step * (
        0.5 * 0.254829592
        + step
        * (
            0.5 * -0.284496736
            + step
            * (0.5 * 1.421413741 + step * (0.5 * -1.453152027 + step * (0.5 * 1.061405429)))
        )
    )
    tail = tail * bell
    share = jnp.where(values >= 0.0, 1.0 - tail, tail)
    return (values * share, share + values * (bell * 0.3989422804014327))


def fold(values):
    chans = values.shape[-1]
    return jnp.sum(values.reshape(-1, 8, chans), axis=0)


def by_image(total):
    total = total + pltpu.roll(total, 4, 0)
    total = total + pltpu.roll(total, 2, 0)
    return jnp.sum(total, axis=1, keepdims=True)


def line(pattern):
    return jnp.concatenate([pattern] * (LINE // 8), axis=0)


def spread(pattern, chans):
    return line(jnp.broadcast_to(pattern, (8, chans)))


def from_left(values):
    flat = values.reshape(-1, values.shape[-1])
    return pltpu.roll(flat, 2, 0).reshape(values.shape)


def from_right(values):
    flat = values.reshape(-1, values.shape[-1])
    return pltpu.roll(flat, flat.shape[0] - 2, 0).reshape(values.shape)


def rounded(values):
    return values.astype(bf16).astype(f32)


def widen(values):
    return jnp.concatenate([values] * (WIDE // 128), axis=-1)


def norm_terms(total, square, count):
    mean = by_image(total) / count
    scaling = lax.rsqrt(by_image(square) / count - mean * mean + eps_norm)
    return (mean, scaling)


def main_kernel(
    pairs,
    strip_count,
    slots,
    extra,
    piece_count,
    slot_ref,
    place_ref,
    size_ref,
    strips_ref,
    goal_ref,
    vec_two_ref,
    vec_hid_two_ref,
    vec_three_ref,
    vec_hid_three_ref,
    *refs,
):
    inner_kernel(
        pairs,
        strip_count,
        slots,
        extra,
        slot_ref,
        place_ref,
        size_ref,
        strips_ref,
        goal_ref,
        vec_two_ref,
        vec_hid_two_ref,
        vec_three_ref,
        vec_hid_three_ref,
        refs[:piece_count],
        *refs[piece_count:],
    )


def inner_kernel(
    pairs,
    strip_count,
    slots,
    extra,
    slot_ref,
    place_ref,
    size_ref,
    strips_ref,
    goal_ref,
    vec_two_ref,
    vec_hid_two_ref,
    vec_three_ref,
    vec_hid_three_ref,
    piece_refs,
    result_ref,
    pixel_ref,
    near_ref,
    far_ref,
    gathered_ref,
    grad_ref,
    strips,
    line_tmp,
    x_ref,
    inv_ref,
    col_ref,
    pool_ref,
    mix_ref,
    zed_ref,
    dx_ref,
    u_ref,
    g_ref,
    h_ref,
    dy_ref,
    patch_ref,
    dpatch_ref,
    inv3_ref,
    e_ref,
    col3_ref,
    pool3_ref,
    mix3_ref,
    dx3_ref,
    u3_ref,
    g3_ref,
    h3_ref,
    dy3_ref,
    dpre_ref,
    w1_ref,
    w2_ref,
    we_ref,
    w3_ref,
    w4_ref,
    gw1_ref,
    gw2_ref,
    gwe_ref,
    gw3_ref,
    gw4_ref,
    acc_two,
    acc_hid_two,
    acc_three,
    acc_hid_three,
    flat_ref,
    in_sem,
    out_sem,
    piece_sem,
    grad_sem,
):
    pair = pl.program_id(0)
    weights = [w1_ref, w2_ref, we_ref, w3_ref, w4_ref]
    grads = [gw1_ref, gw2_ref, gwe_ref, gw3_ref, gw4_ref]

    def strip_copies(outward):
        copies = []
        for half in range(4):
            start = lax.rem(pair * 8 + strip_count - 2 + 2 * half, strip_count)
            inside = strips.at[pl.ds(2 * half, 2)]
            if outward:
                copies.append(
                    pltpu.make_async_copy(inside, pixel_ref.at[pl.ds(start, 2)], out_sem.at[half])
                )
            else:
                copies.append(
                    pltpu.make_async_copy(strips_ref.at[pl.ds(start, 2)], inside, in_sem.at[half])
                )
        return copies

    for copy in strip_copies(False):
        copy.start()

    left_half = lax.broadcasted_iota(jnp.int32, (HALF, 128), 1) < BS

    def piece_copies():
        count = slots // len(piece_refs)
        return [
            pltpu.make_async_copy(
                ref, gathered_ref.at[pl.ds(n * count, count)], piece_sem.at[n]
            )
            for n, ref in enumerate(piece_refs)
        ]

    def grad_copies():
        half = grad_ref.shape[0] // 2
        return [
            pltpu.make_async_copy(grad_ref.at[pl.ds(n * half, half)], ref, grad_sem.at[n])
            for n, ref in enumerate((near_ref, far_ref))
        ]

    def unpack():
        for copy in piece_copies():
            copy.wait()
        offset = 0
        for (rows, cols), ref in zip(SHAPES, weights):
            wide = cols // BS
            for rb in range(rows // BS):
                for cb in range(0, wide, 2):
                    number = offset + rb * wide + cb
                    first = gathered_ref[slot_ref[number]].astype(f32)
                    turned = pltpu.roll(first, BS, 1)
                    if cb + 1 < wide:
                        second = gathered_ref[slot_ref[number + 1]].astype(f32)
                        top = jnp.where(left_half, first, pltpu.roll(second, BS, 1))
                        low = jnp.where(left_half, turned, second)
                    else:
                        top = jnp.where(left_half, first, 0.0)
                        low = jnp.where(left_half, turned, 0.0)
                    place = slice(cb * BS, cb * BS + 128)
                    ref[rb * BS : rb * BS + HALF, place] = top.astype(bf16)
                    ref[rb * BS + HALF : rb * BS + BS, place] = low.astype(bf16)
            offset += rows // BS * wide
        w3_ref[C3:, :] = jnp.zeros((WIDE - C3, HID3), bf16)

    @pl.when(pair == 0)
    def _():
        for copy in piece_copies():
            copy.start()
        unpack()
        acc_two[...] = jnp.zeros(acc_two.shape, f32)
        acc_hid_two[...] = jnp.zeros(acc_hid_two.shape, f32)
        acc_three[...] = jnp.zeros(acc_three.shape, f32)
        acc_hid_three[...] = jnp.zeros(acc_hid_three.shape, f32)

    parity = lax.broadcasted_iota(jnp.int32, (8, 128), 0) % 2
    high = jnp.where(parity == 0, size_ref[pair * 4], size_ref[pair * 4 + 2])
    broad = jnp.where(parity == 0, size_ref[pair * 4 + 1], size_ref[pair * 4 + 3])
    count_two = (high * broad * C2).astype(f32)[:, :1]
    high3 = (high + 1) // 2
    broad3 = (broad + 1) // 2
    count_three = (high3 * broad3 * C3).astype(f32)[:, :1]
    place = lax.broadcasted_iota(jnp.int32, (LINE, 128), 0) // 2
    inside = lax.broadcasted_iota(jnp.int32, (LINE, 128), 0) < 2 * W3
    reach = []
    col_share = []
    for pc in range(2):
        column = 2 * place + pc
        reach.append(jnp.where(inside & (column < line(broad)), line(high), 0))
        edge = (column == 0) | (column == line(broad) - 1)
        col_share.append(jnp.where(edge, 0.5, 1.0 / 3.0))
    reach3 = jnp.where(inside & (place < line(broad3)), line(high3), 0)
    edge3 = (place == 0) | (place == line(broad3) - 1)
    col_share3 = jnp.where(edge3, 0.5, 1.0 / 3.0)

    def row_share(row, height):
        return jnp.where((row == 0) | (row == height - 1), 0.5, 1.0 / 3.0)

    gain1, bias1, scale1 = (vec_two_ref[n : n + 1] for n in range(3))
    gain2, bias2, scale2, out_bias = (vec_two_ref[n : n + 1] for n in range(3, 7))
    embed_bias, gain3, bias3, scale3 = (vec_three_ref[n : n + 1] for n in range(4))
    gain4, bias4, scale4, out_bias3 = (vec_three_ref[n : n + 1] for n in range(4, 8))

    for copy in strip_copies(False):
        copy.wait()

    zero_line = jnp.zeros((1, LINE, C2), f32)
    zero_line3 = jnp.zeros((1, LINE, WIDE), f32)
    for plane in range(4):
        col_ref[plane, 0:1] = zero_line
        col_ref[plane, H3 + 1 : H3 + 2] = zero_line
        zed_ref[plane, 0:1] = zero_line
    col3_ref[0:1] = zero_line3
    col3_ref[H3 + 1 : H3 + 2] = zero_line3

    def arrange(r, carry):
        total, square = carry
        for pr in range(2):
            row = 2 * r + pr
            strip = row // SR
            within = row - strip * SR
            for image in range(2):
                spot = pr * 2 + image
                line_tmp[spot, 0:CW] = strips[image * STRIPS + strip, within].astype(f32)
                for pc in range(2):
                    x_ref[pr * 2 + pc, r, pl.ds(image, W3, stride=2)] = line_tmp[
                        spot, pl.ds(pc, W3, stride=2)
                    ]
            for pc in range(2):
                plane = pr * 2 + pc
                valid = row < reach[pc]
                inv_ref[plane, r] = jnp.where(
                    valid, line(row_share(row, high)) * col_share[pc], 0.0
                )
                values = jnp.where(valid, x_ref[plane, r], 0.0)
                x_ref[plane, r] = values
                total = total + fold(values)
                square = square + fold(values * values)
        inv3_ref[r] = jnp.where(r < reach3, line(row_share(r, high3)) * col_share3, 0.0)
        return (total, square)

    nothing = jnp.zeros((8, C2), f32)
    nothing3 = jnp.zeros((8, WIDE), f32)
    total, square = lax.fori_loop(0, H3, arrange, (nothing, nothing))
    mean1, scaling1 = norm_terms(total, square, count_two)
    factor1 = line(scaling1 * gain1)
    shift1 = line(bias1 - mean1 * scaling1 * gain1)

    def window_cols(k, carry):
        rows = pl.ds(2 * k, 2)
        for pr in range(2):
            masked = []
            for pc in range(2):
                plane = pr * 2 + pc
                normal = rounded(x_ref[plane, rows] * factor1 + shift1)
                masked.append(jnp.where(inv_ref[plane, rows] > 0.0, normal, 0.0))
            both = masked[0] + masked[1]
            col_ref[pr * 2, pl.ds(2 * k + 1, 2)] = both + from_left(masked[1])
            col_ref[pr * 2 + 1, pl.ds(2 * k + 1, 2)] = both + from_right(masked[0])
        return carry

    lax.fori_loop(0, H3 // 2, window_cols, 0)

    def row_windows(pc, k):
        even = col_ref[pc, pl.ds(2 * k + 1, 2)]
        odd = col_ref[2 + pc, pl.ds(2 * k + 1, 2)]
        both = even + odd
        return (both + col_ref[2 + pc, pl.ds(2 * k, 2)], both + col_ref[pc, pl.ds(2 * k + 2, 2)])

    def mix(k, carry):
        total, square = carry
        rows = pl.ds(2 * k, 2)
        for pc in range(2):
            windows = row_windows(pc, k)
            for pr in range(2):
                plane = pr * 2 + pc
                values = x_ref[plane, rows]
                share = inv_ref[plane, rows]
                pooled = windows[pr] * share - rounded(values * factor1 + shift1)
                pooled = jnp.where(share > 0.0, pooled, 0.0)
                mixed = values + scale1 * pooled
                pool_ref[plane, rows] = pooled
                mix_ref[plane, rows] = mixed
                total = total + fold(mixed)
                square = square + fold(mixed * mixed)
        return (total, square)

    total, square = lax.fori_loop(0, H3 // 2, mix, (nothing, nothing))
    mean2, scaling2 = norm_terms(total, square, count_two)
    factor2 = line(scaling2 * gain2)
    shift2 = line(bias2 - mean2 * scaling2 * gain2)

    def where_chunk(c):
        plane = c // STEPS
        first = (c - plane * STEPS) * ROWS
        return (plane, first, pl.ds(pl.multiple_of(c * CHUNK, CHUNK), CHUNK))

    def branch(c, carry):
        plane, first, flat = where_chunk(c)
        mixed = mix_ref[plane, pl.ds(first, ROWS)]
        low = (mixed * factor2 + shift2).reshape(CHUNK, C2).astype(bf16)
        h_ref[flat] = low
        hidden = product(low, w1_ref[...]) + vec_hid_two_ref[...]
        active, slope = gelu_pair(hidden)
        active = active.astype(bf16)
        u_ref[flat] = active
        g_ref[flat] = slope.astype(bf16)
        out = (product(active, w2_ref[...]) + out_bias).reshape(ROWS, LINE, C2)
        valid = inv_ref[plane, pl.ds(first, ROWS)] > 0.0
        zed = rounded(jnp.where(valid, mixed + scale2 * out, 0.0))
        zed_ref[plane, pl.ds(first + 1, ROWS)] = zed
        return carry

    lax.fori_loop(0, 4 * STEPS, branch, 0)

    def patches(k, carry):
        flat = pl.ds(pl.multiple_of(k * 2 * LINE, 2 * LINE), 2 * LINE)
        for ky in range(3):
            pr = (0 if ky == 1 else 1) * 2
            rows = pl.ds(2 * k + (0 if ky == 0 else 1), 2)
            even = zed_ref[pr, rows]
            odd = zed_ref[pr + 1, rows]
            for kx, tap in enumerate((from_left(odd), even, odd)):
                at = (3 * ky + kx) * C2
                patch_ref[flat, at : at + C2] = tap.reshape(2 * LINE, C2).astype(bf16)
        return carry

    lax.fori_loop(0, H3 // 2, patches, 0)

    def embed(c, carry):
        total, square = carry
        flat = pl.ds(pl.multiple_of(c * CHUNK, CHUNK), CHUNK)
        rows = pl.ds(c * ROWS, ROWS)
        out = (product(patch_ref[flat], we_ref[...]) + embed_bias).reshape(ROWS, LINE, WIDE)
        out = jnp.where(widen(inv3_ref[rows]) > 0.0, out, 0.0)
        e_ref[rows] = out
        return (total + fold(out), square + fold(out * out))

    total, square = lax.fori_loop(0, STEPS, embed, (nothing3, nothing3))
    mean3, scaling3 = norm_terms(total, square, count_three)
    factor3 = line(scaling3 * gain3)
    shift3 = line(bias3 - mean3 * scaling3 * gain3)

    def window_cols3(k, carry):
        rows = pl.ds(2 * k, 2)
        normal = rounded(e_ref[rows] * factor3 + shift3)
        masked = jnp.where(widen(inv3_ref[rows]) > 0.0, normal, 0.0)
        col3_ref[pl.ds(2 * k + 1, 2)] = masked + from_left(masked) + from_right(masked)
        return carry

    lax.fori_loop(0, H3 // 2, window_cols3, 0)

    def row_windows3(k):
        return (
            col3_ref[pl.ds(2 * k, 2)]
            + col3_ref[pl.ds(2 * k + 1, 2)]
            + col3_ref[pl.ds(2 * k + 2, 2)]
        )

    def mix3(k, carry):
        total, square = carry
        rows = pl.ds(2 * k, 2)
        values = e_ref[rows]
        share = widen(inv3_ref[rows])
        pooled = row_windows3(k) * share - rounded(values * factor3 + shift3)
        pooled = jnp.where(share > 0.0, pooled, 0.0)
        mixed = values + scale3 * pooled
        pool3_ref[rows] = pooled
        mix3_ref[rows] = mixed
        return (total + fold(mixed), square + fold(mixed * mixed))

    total, square = lax.fori_loop(0, H3 // 2, mix3, (nothing3, nothing3))
    mean4, scaling4 = norm_terms(total, square, count_three)
    factor4 = line(scaling4 * gain4)
    shift4 = line(bias4 - mean4 * scaling4 * gain4)
    normal4 = (spread(scaling4, WIDE), spread(-mean4 * scaling4, WIDE))

    def branch3(c, carry):
        d_out_bias, d_scale, d_hidden_bias, d_shift, d_gain = carry
        flat = pl.ds(pl.multiple_of(c * CHUNK, CHUNK), CHUNK)
        rows = pl.ds(c * ROWS, ROWS)
        mixed = mix3_ref[rows]
        low = (mixed * factor4 + shift4).reshape(CHUNK, WIDE).astype(bf16)
        h3_ref[flat] = low
        hidden = product(low, w3_ref[...]) + vec_hid_three_ref[...]
        active, slope = gelu_pair(hidden)
        active = active.astype(bf16)
        u3_ref[flat] = active
        out = (product(active, w4_ref[...]) + out_bias3).reshape(ROWS, LINE, WIDE)
        valid = widen(inv3_ref[rows]) > 0.0
        out = jnp.where(valid, out, 0.0)
        result_ref[0, rows] = mixed + scale4 * out
        goal = jnp.where(valid, goal_ref[0, flat].astype(f32).reshape(ROWS, LINE, WIDE), 0.0)
        low_goal = (scale4 * goal).reshape(CHUNK, WIDE).astype(bf16)
        dy3_ref[flat] = low_goal
        d_hidden = (slope * product_nt(low_goal, w4_ref[...])).astype(bf16)
        g3_ref[flat] = d_hidden
        d_low = product_nt(d_hidden, w3_ref[...]).reshape(ROWS, LINE, WIDE)
        dx3_ref[rows] = d_low
        normal = mixed * normal4[0] + normal4[1]
        return (
            d_out_bias + fold(low_goal.astype(f32)),
            d_scale + fold(out * goal),
            d_hidden_bias + fold(d_hidden.astype(f32)),
            d_shift + fold(d_low),
            d_gain + fold(d_low * normal),
        )

    wide_zero = jnp.zeros((8, HID3), f32)
    d_out_bias, d_scale, d_hidden_bias, d_shift, d_gain = lax.fori_loop(
        0, STEPS, branch3, (nothing3, nothing3, wide_zero, nothing3, nothing3)
    )
    acc_three[7] += d_out_bias
    acc_three[6] += d_scale
    acc_hid_three[...] += d_hidden_bias
    acc_three[5] += d_shift
    acc_three[4] += d_gain
    mean_shift = by_image(d_shift * gain4) / count_three
    mean_gain = by_image(d_gain * gain4) / count_three

    def keep(ref, value):
        if pairs == 1:
            ref[...] = value
        else:

            @pl.when(pair == 0)
            def _():
                ref[...] = value

            @pl.when(pair > 0)
            def _():
                ref[...] += value

    keep(gw3_ref, product_tn(h3_ref[...], g3_ref[...]))
    keep(gw4_ref, product_tn(u3_ref[...], dy3_ref[...]))

    back_gain4 = line(scaling4 * gain4)
    back_mean4 = spread(scaling4 * mean_shift, WIDE)
    back_normal4 = spread(scaling4 * mean_gain, WIDE)

    def unmix3(k, d_scale):
        rows = pl.ds(2 * k, 2)
        flat = pl.ds(pl.multiple_of(k * 2 * LINE, 2 * LINE), 2 * LINE)
        share = widen(inv3_ref[rows])
        valid = share > 0.0
        normal = mix3_ref[rows] * normal4[0] + normal4[1]
        back = dx3_ref[rows] * back_gain4 - back_mean4 - normal * back_normal4
        goal = goal_ref[0, flat].astype(f32).reshape(2, LINE, WIDE)
        d_mixed = jnp.where(valid, back + goal, 0.0)
        dx3_ref[rows] = d_mixed
        d_scale = d_scale + fold(pool3_ref[rows] * d_mixed)
        weighted = scale3 * d_mixed * share
        col3_ref[pl.ds(2 * k + 1, 2)] = weighted + from_left(weighted) + from_right(weighted)
        return d_scale

    acc_three[3] += lax.fori_loop(0, H3 // 2, unmix3, nothing3)
    normal3 = (spread(scaling3, WIDE), spread(-mean3 * scaling3, WIDE))

    def unpool3(k, carry):
        d_shift, d_gain = carry
        rows = pl.ds(2 * k, 2)
        valid = widen(inv3_ref[rows]) > 0.0
        d_normal = jnp.where(valid, row_windows3(k) - scale3 * dx3_ref[rows], 0.0)
        pool3_ref[rows] = d_normal
        normal = e_ref[rows] * normal3[0] + normal3[1]
        return (d_shift + fold(d_normal), d_gain + fold(d_normal * normal))

    d_shift, d_gain = lax.fori_loop(0, H3 // 2, unpool3, (nothing3, nothing3))
    acc_three[2] += d_shift
    acc_three[1] += d_gain
    mean_shift = by_image(d_shift * gain3) / count_three
    mean_gain = by_image(d_gain * gain3) / count_three
    back_gain3 = line(scaling3 * gain3)
    back_mean3 = spread(scaling3 * mean_shift, WIDE)
    back_normal3 = spread(scaling3 * mean_gain, WIDE)

    def unnorm3(k, d_bias):
        rows = pl.ds(2 * k, 2)
        flat = pl.ds(pl.multiple_of(k * 2 * LINE, 2 * LINE), 2 * LINE)
        valid = widen(inv3_ref[rows]) > 0.0
        normal = e_ref[rows] * normal3[0] + normal3[1]
        back = pool3_ref[rows] * back_gain3 - back_mean3 - normal * back_normal3
        low = jnp.where(valid, dx3_ref[rows] + back, 0.0).astype(bf16)
        dpre_ref[flat] = low.reshape(2 * LINE, WIDE)
        return d_bias + fold(low.astype(f32))

    acc_three[0] += lax.fori_loop(0, H3 // 2, unnorm3, nothing3)
    keep(gwe_ref, product_tn(patch_ref[...], dpre_ref[...]))

    def unpatch(c, carry):
        flat = pl.ds(pl.multiple_of(c * CHUNK, CHUNK), CHUNK)
        rows = pl.ds(c * ROWS, ROWS)
        dpatch_ref[rows] = product_nt(dpre_ref[flat], we_ref[...]).reshape(ROWS, LINE, 9 * C2)
        return carry

    lax.fori_loop(0, STEPS, unpatch, 0)
    dpatch_ref[H3 : H3 + 1] = jnp.zeros((1, LINE, 9 * C2), f32)

    def tap(ky, kx, rows):
        at = (3 * ky + kx) * C2
        return dpatch_ref[rows, :, at : at + C2]

    def gather_back(k, carry):
        here = pl.ds(2 * k, 2)
        below = pl.ds(2 * k + 1, 2)
        sources = []
        for ky, rows in ((0, below), (1, here), (2, here)):
            sources.append((tap(ky, 1, rows), tap(ky, 2, rows) + from_right(tap(ky, 0, rows))))
        for pc in range(2):
            for pr, value in ((0, sources[1][pc]), (1, sources[2][pc] + sources[0][pc])):
                plane = pr * 2 + pc
                valid = inv_ref[plane, here] > 0.0
                zed_ref[plane, here] = jnp.where(valid, rounded(value), 0.0)
        return carry

    lax.fori_loop(0, H3 // 2, gather_back, 0)

    normal2 = (spread(scaling2, C2), spread(-mean2 * scaling2, C2))

    def unbranch(c, carry):
        d_out_bias, d_hidden_bias, d_shift, d_gain = carry
        plane, first, flat = where_chunk(c)
        rows = pl.ds(first, ROWS)
        low_goal = (scale2 * zed_ref[plane, rows]).reshape(CHUNK, C2).astype(bf16)
        dy_ref[flat] = low_goal
        d_hidden = g_ref[flat].astype(f32) * product_nt(low_goal, w2_ref[...])
        d_hidden = d_hidden.astype(bf16)
        g_ref[flat] = d_hidden
        d_low = product_nt(d_hidden, w1_ref[...]).reshape(ROWS, LINE, C2)
        dx_ref[plane, rows] = d_low
        normal = mix_ref[plane, rows] * normal2[0] + normal2[1]
        return (
            d_out_bias + fold(low_goal.astype(f32)),
            d_hidden_bias + fold(d_hidden.astype(f32)),
            d_shift + fold(d_low),
            d_gain + fold(d_low * normal),
        )

    d_out_bias, d_hidden_bias, d_shift, d_gain = lax.fori_loop(
        0, 4 * STEPS, unbranch, (nothing, jnp.zeros((8, HID2), f32), nothing, nothing)
    )
    acc_two[6] += d_out_bias
    acc_hid_two[...] += d_hidden_bias
    acc_two[4] += d_shift
    acc_two[3] += d_gain
    mean_shift = by_image(d_shift * gain2) / count_two
    mean_gain = by_image(d_gain * gain2) / count_two
    keep(gw1_ref, product_tn(h_ref[...], g_ref[...]))
    new_gw2 = product_tn(dy_ref[...], u_ref[...]).T
    keep(gw2_ref, new_gw2)
    d_scale = fold(w2_ref[...].astype(f32) * new_gw2) + out_bias * d_out_bias
    acc_two[5] += d_scale / scale2

    back_gain2 = line(scaling2 * gain2)
    back_mean2 = spread(scaling2 * mean_shift, C2)
    back_normal2 = spread(scaling2 * mean_gain, C2)

    def unmix(k, d_scale):
        rows = pl.ds(2 * k, 2)
        for pr in range(2):
            weighted = []
            for pc in range(2):
                plane = pr * 2 + pc
                share = inv_ref[plane, rows]
                normal = mix_ref[plane, rows] * normal2[0] + normal2[1]
                back = dx_ref[plane, rows] * back_gain2 - back_mean2 - normal * back_normal2
                d_mixed = jnp.where(share > 0.0, zed_ref[plane, rows] + back, 0.0)
                dx_ref[plane, rows] = d_mixed
                d_scale = d_scale + fold(pool_ref[plane, rows] * d_mixed)
                weighted.append(scale1 * d_mixed * share)
            both = weighted[0] + weighted[1]
            col_ref[pr * 2, pl.ds(2 * k + 1, 2)] = both + from_left(weighted[1])
            col_ref[pr * 2 + 1, pl.ds(2 * k + 1, 2)] = both + from_right(weighted[0])
        return d_scale

    acc_two[2] += lax.fori_loop(0, H3 // 2, unmix, nothing)
    normal1 = (spread(scaling1, C2), spread(-mean1 * scaling1, C2))

    def unpool(k, carry):
        d_shift, d_gain = carry
        rows = pl.ds(2 * k, 2)
        for pc in range(2):
            windows = row_windows(pc, k)
            for pr in range(2):
                plane = pr * 2 + pc
                valid = inv_ref[plane, rows] > 0.0
                d_normal = windows[pr] - scale1 * dx_ref[plane, rows]
                d_normal = jnp.where(valid, d_normal, 0.0)
                pool_ref[plane, rows] = d_normal
                normal = x_ref[plane, rows] * normal1[0] + normal1[1]
                d_shift = d_shift + fold(d_normal)
                d_gain = d_gain + fold(d_normal * normal)
        return (d_shift, d_gain)

    d_shift, d_gain = lax.fori_loop(0, H3 // 2, unpool, (nothing, nothing))
    acc_two[1] += d_shift
    acc_two[0] += d_gain
    mean_shift = by_image(d_shift * gain1) / count_two
    mean_gain = by_image(d_gain * gain1) / count_two
    back_gain1 = line(scaling1 * gain1)
    back_mean1 = spread(scaling1 * mean_shift, C2)
    back_normal1 = spread(scaling1 * mean_gain, C2)

    def unnorm(r, carry):
        for pr in range(2):
            row = 2 * r + pr
            strip = row // SR
            within = row - strip * SR
            for pc in range(2):
                plane = pr * 2 + pc
                normal = x_ref[plane, r] * normal1[0] + normal1[1]
                back = pool_ref[plane, r] * back_gain1 - back_mean1 - normal * back_normal1
                dx_ref[plane, r] = jnp.where(
                    inv_ref[plane, r] > 0.0, dx_ref[plane, r] + back, 0.0
                )
            for image in range(2):
                spot = pr * 2 + image
                for pc in range(2):
                    line_tmp[spot, pl.ds(pc, W3, stride=2)] = dx_ref[
                        pr * 2 + pc, r, pl.ds(image, W3, stride=2)
                    ]
                strips[image * STRIPS + strip, within] = line_tmp[spot, 0:CW].astype(bf16)
        return carry

    lax.fori_loop(0, H3, unnorm, 0)
    for copy in strip_copies(True):
        copy.start()

    @pl.when(pair == pairs - 1)
    def _():
        offset = 0
        for (rows, cols), ref in zip(SHAPES, grads):
            wide = cols // BS
            for rb in range(rows // BS):
                for cb in range(0, wide, 2):
                    number = offset + rb * wide + cb
                    at = slice(cb * BS, cb * BS + 128)
                    top = ref[rb * BS : rb * BS + HALF, at]
                    low = ref[rb * BS + HALF : rb * BS + BS, at]
                    grad_ref[place_ref[number]] = jnp.where(
                        left_half, top, pltpu.roll(low, BS, 1)
                    ).astype(bf16)
                    if cb + 1 < wide:
                        grad_ref[place_ref[number + 1]] = jnp.where(
                            left_half, pltpu.roll(top, BS, 1), low
                        ).astype(bf16)
            offset += rows // BS * wide

        def filler(number, carry):
            grad_ref[place_ref[number]] = jnp.zeros((HALF, 128), bf16)
            return carry

        lax.fori_loop(USED, slots, filler, 0)

        flat_ref[...] = jnp.zeros(flat_ref.shape, f32)

        def put(at, total, length):
            if at % 128:
                room = jnp.zeros((8, 128), f32)
                if total.shape[1] < length + BS:
                    total = jnp.concatenate([total, room], axis=1)
                total = pltpu.roll(total, BS, 1)
            whole = jnp.sum(total, axis=0, keepdims=True)
            done = -(at % 128)
            row = at // 128
            lane = 0
            while done < length:
                first = max(0, -done)
                last = min(128, length - done)
                flat_ref[row : row + 1, first:last] = whole[:, lane + first : lane + last]
                done += 128
                lane += 128
                row += 1

        at = 0
        for n in range(6):
            put(at, acc_two[n], C2)
            at += C2
        put(at, acc_hid_two[...], HID2)
        at += HID2
        put(at, acc_two[6], C2)
        at += C2
        for n in range(7):
            put(at, acc_three[n], C3)
            at += C3
        put(at, acc_hid_three[...], HID3)
        at += HID3
        put(at, acc_three[7], C3)
        packed = flat_ref[...].astype(bf16)
        stride = slots // strip_count + extra
        for n in range(extra):
            piece = packed[n * HALF : (n + 1) * HALF]

            def leave(target, carry):
                grad_ref[target * stride + stride - extra + n] = piece
                return carry

            lax.fori_loop(0, strip_count, leave, 0)
        for copy in grad_copies():
            copy.start()
        for copy in grad_copies():
            copy.wait()

    for copy in strip_copies(True):
        copy.wait()


def run_main(slot_of, place_of, sizes, strips, goal, vectors, pieces, extra):
    strip_count = strips.shape[0]
    pairs = goal.shape[0]
    slots = sum(piece.shape[0] for piece in pieces)
    rows_out = slots + extra * strip_count

    def whole(shape):
        return pl.BlockSpec(shape, lambda t: (0,) * len(shape), pipeline_mode=pl.Buffered(1))

    smem = pl.BlockSpec(memory_space=pltpu.SMEM)
    anywhere = pl.BlockSpec(memory_space=pl.ANY)
    plane_f32 = pltpu.VMEM((4, H3, LINE, C2), f32)
    wide_f32 = pltpu.VMEM((H3, LINE, WIDE), f32)
    scratch = [
        pltpu.VMEM((slots, HALF, 128), bf16),
        pltpu.VMEM((rows_out, HALF, 128), bf16),
        pltpu.VMEM((2 * STRIPS, SR, CW, C2), bf16),
        pltpu.VMEM((4, LINE, C2), f32),
        plane_f32,
        plane_f32,
        pltpu.VMEM((4, H3 + 2, LINE, C2), f32),
        plane_f32,
        plane_f32,
        pltpu.VMEM((4, H3 + 1, LINE, C2), f32),
        plane_f32,
        pltpu.VMEM((4 * PLANE, HID2), bf16),
        pltpu.VMEM((4 * PLANE, HID2), bf16),
        pltpu.VMEM((4 * PLANE, C2), bf16),
        pltpu.VMEM((4 * PLANE, C2), bf16),
        pltpu.VMEM((PLANE, 9 * C2), bf16),
        pltpu.VMEM((H3 + 1, LINE, 9 * C2), f32),
        pltpu.VMEM((H3, LINE, 128), f32),
        wide_f32,
        pltpu.VMEM((H3 + 2, LINE, WIDE), f32),
        wide_f32,
        wide_f32,
        wide_f32,
        pltpu.VMEM((PLANE, HID3), bf16),
        pltpu.VMEM((PLANE, HID3), bf16),
        pltpu.VMEM((PLANE, WIDE), bf16),
        pltpu.VMEM((PLANE, WIDE), bf16),
        pltpu.VMEM((PLANE, WIDE), bf16),
        pltpu.VMEM((C2, HID2), bf16),
        pltpu.VMEM((HID2, C2), bf16),
        pltpu.VMEM((9 * C2, WIDE), bf16),
        pltpu.VMEM((WIDE, HID3), bf16),
        pltpu.VMEM((HID3, WIDE), bf16),
        pltpu.VMEM((C2, HID2), f32),
        pltpu.VMEM((HID2, C2), f32),
        pltpu.VMEM((9 * C2, WIDE), f32),
        pltpu.VMEM((WIDE, HID3), f32),
        pltpu.VMEM((HID3, WIDE), f32),
        pltpu.VMEM((7, 8, C2), f32),
        pltpu.VMEM((8, HID2), f32),
        pltpu.VMEM((8, 8, WIDE), f32),
        pltpu.VMEM((8, HID3), f32),
        pltpu.VMEM((extra * HALF, 128), f32),
        pltpu.SemaphoreType.DMA((4,)),
        pltpu.SemaphoreType.DMA((4,)),
        pltpu.SemaphoreType.DMA((len(pieces),)),
        pltpu.SemaphoreType.DMA((2,)),
    ]
    return pl.pallas_call(
        functools.partial(main_kernel, pairs, strip_count, slots, extra, len(pieces)),
        grid=(pairs,),
        in_specs=[
            smem,
            smem,
            smem,
            anywhere,
            pl.BlockSpec((1,) + goal.shape[1:], lambda t: (t, 0, 0)),
        ]
        + [whole(vector.shape) for vector in vectors]
        + [anywhere] * len(pieces),
        out_specs=[
            pl.BlockSpec((1, H3, LINE, WIDE), lambda t: (t, 0, 0, 0)),
            anywhere,
            anywhere,
            anywhere,
        ],
        out_shape=[
            jax.ShapeDtypeStruct((pairs, H3, LINE, WIDE), f32),
            jax.ShapeDtypeStruct(strips.shape, bf16),
            jax.ShapeDtypeStruct((rows_out // 2, HALF, 128), bf16),
            jax.ShapeDtypeStruct((rows_out // 2, HALF, 128), bf16),
        ],
        scratch_shapes=scratch,
        compiler_params=pltpu.CompilerParams(vmem_limit_bytes=62 * 1024 * 1024),
        name="blocks",
    )(slot_of, place_of, sizes, strips, goal, *vectors, *pieces)


def pack_kernel(master_ref, dense_ref):
    values = master_ref[...]
    dense_ref[...] = jnp.concatenate([values[:, :HALF], values[:, HALF:]], axis=2).astype(bf16)


def pack(master):
    owned = master.shape[0]
    return pl.pallas_call(
        pack_kernel,
        out_shape=jax.ShapeDtypeStruct((owned, HALF, 2 * BS), bf16),
        name="pack",
    )(master)


def fold_pair_kernel(near_ref, got_ref, own_ref, *part_refs):
    for n in range(len(part_refs) + 1):
        total = near_ref[n].astype(f32) + got_ref[n].astype(f32)
        if n == 0:
            own_ref[...] = total
        else:
            part_refs[n - 1][...] = total.astype(bf16)


def fold_pair(near, got):
    part = jax.ShapeDtypeStruct(near.shape[1:], bf16)
    own = jax.ShapeDtypeStruct(near.shape[1:], f32)
    return pl.pallas_call(
        fold_pair_kernel,
        out_shape=[own] + [part] * (near.shape[0] - 1),
        name="fold_pair",
    )(near, got)


def fold_tile_kernel(pieces, spot_ref, *refs):
    piece_refs, (own_ref, *part_refs) = refs[:pieces], refs[pieces:]
    groups = len(part_refs) + 1
    share = own_ref.shape[0]
    for k in range(groups):
        start = lax.rem(spot_ref[0] + k, groups) * share
        total = piece_refs[0][pl.ds(start, share)].astype(f32)
        for ref in piece_refs[1:]:
            total = total + ref[pl.ds(start, share)].astype(f32)
        if k == 0:
            own_ref[...] = total
        else:
            part_refs[k - 1][...] = total.astype(bf16)


def fold_tile(spot, pieces, groups):
    share = pieces[0].shape[0] // groups
    part = jax.ShapeDtypeStruct((share,) + pieces[0].shape[1:], bf16)
    own = jax.ShapeDtypeStruct(part.shape, f32)
    return pl.pallas_call(
        functools.partial(fold_tile_kernel, len(pieces)),
        in_specs=[pl.BlockSpec(memory_space=pltpu.SMEM)]
        + [pl.BlockSpec(memory_space=pltpu.VMEM)] * len(pieces),
        out_shape=[own] + [part] * (groups - 1),
        name="fold_tile",
    )(spot, *pieces)


def fold_batch_kernel(owned, vector_weight, spot_ref, own_ref, *refs):
    part_refs, (total_ref, norm_ref) = refs[:-2], refs[-2:]
    share = own_ref.shape[0]
    square = jnp.zeros((8, 128), f32)
    for n in range(share):
        total = own_ref[n]
        for ref in part_refs:
            total = total + ref[n].astype(f32)
        total_ref[n] = total.astype(bf16)
        weight = jnp.where(spot_ref[0] * share + n < owned, 1.0, vector_weight)
        square = square + weight * fold(total * total)
    square = jnp.sum(jnp.sum(square, axis=1, keepdims=True), axis=0, keepdims=True)
    norm_ref[...] = jnp.broadcast_to(square[None], norm_ref.shape)


def fold_batch(spot, own, parts, owned, tile_count):
    count = tile_count * (len(parts) + 1)
    vmem = pl.BlockSpec(memory_space=pltpu.VMEM)
    return pl.pallas_call(
        functools.partial(fold_batch_kernel, owned, 1.0 / tile_count),
        in_specs=[pl.BlockSpec(memory_space=pltpu.SMEM)] + [vmem] * (len(parts) + 1),
        out_shape=[
            jax.ShapeDtypeStruct(own.shape, bf16),
            jax.ShapeDtypeStruct((count, 1, 128), f32),
        ],
        name="fold_batch",
    )(spot, own, *parts)


def update_kernel(owned, groups, spot_ref, norm_ref, *refs):
    quarters = refs[:groups]
    (
        master_ref,
        left_stat_ref,
        right_stat_ref,
        left_root_ref,
        right_root_ref,
        grad_ref,
        left_ref,
        right_ref,
        new_ref,
        copy_ref,
        vector_ref,
        clip_ref,
    ) = refs[groups:]
    share = quarters[0].shape[0]
    part = grad_ref.shape[0]
    step = pl.program_id(0)
    norm = jnp.sqrt(jnp.sum(norm_ref[...], axis=0))
    factor = jnp.minimum(1.0, clip_limit / norm)

    def summed(number):
        source = number // share
        local = number - source * share
        turn = lax.rem(spot_ref[0] - source + groups, groups)
        value = quarters[0][local].astype(f32)
        for k in range(1, groups):
            value = jnp.where(turn == k, quarters[k][local].astype(f32), value)
        return value * factor

    @pl.when(step == 0)
    def _():
        clip_ref[...] = norm
        for n in range(vector_ref.shape[0]):
            vector_ref[n] = summed(owned + n)

    for n in range(part):
        dense = summed(jnp.minimum(step * part + n, owned - 1))
        grad = jnp.concatenate([dense[:, :BS], dense[:, BS:]], axis=0)
        grad_ref[n] = grad
        low = grad.astype(bf16)
        left_ref[n] = 0.5 * left_stat_ref[n] + 0.5 * product_nt(low, low)
        right_ref[n] = 0.5 * right_stat_ref[n] + 0.5 * product_tn(low, low)
        stepped = product(left_root_ref[n].astype(bf16), low).astype(bf16)
        stepped = product(stepped, right_root_ref[n].astype(bf16))
        new = master_ref[n] - rate_matrix * stepped
        new_ref[n] = new
        copy_ref[n] = new.astype(bf16)


def update(spot, norm, quarters, extra, master, *stats):
    owned = master.shape[0]
    part = min(owned, 7)
    groups = len(quarters)
    square = pl.BlockSpec((part, BS, BS), lambda t: (t, 0, 0))
    shape = jax.ShapeDtypeStruct(master.shape, f32)

    def whole(shape):
        return pl.BlockSpec(shape, lambda t: (0,) * len(shape))

    return pl.pallas_call(
        functools.partial(update_kernel, owned, groups),
        grid=(-(-owned // part),),
        in_specs=[pl.BlockSpec(memory_space=pltpu.SMEM), whole(norm.shape)]
        + [whole(quarters[0].shape)] * groups
        + [square] * 5,
        out_specs=[square] * 5 + [whole((extra, HALF, 128)), whole((1, 128))],
        out_shape=[shape] * 4
        + [
            jax.ShapeDtypeStruct(master.shape, bf16),
            jax.ShapeDtypeStruct((extra, HALF, 128), f32),
            jax.ShapeDtypeStruct((1, 128), f32),
        ],
        compiler_params=pltpu.CompilerParams(vmem_limit_bytes=32 * 1024 * 1024),
        name="update",
    )(spot, norm, *quarters, master, *stats)


def share_out(pieces, axis):
    return lax.all_to_all(pieces, axis, split_axis=0, concat_axis=0, tiled=True)


def swap(piece, distance):
    count = lax.axis_size("tile")
    return lax.ppermute(piece, "tile", [(i, i ^ distance) for i in range(count)])


def on_device(
    pixels,
    buckets,
    slot_owner_table,
    out_grad,
    master,
    left_stat,
    right_stat,
    left_root,
    right_root,
    vectors,
    moment,
):
    tile_count = lax.axis_size("tile")
    tile_place = lax.axis_index("tile")
    slot_count = pixels.shape[2]
    group_count = tile_count // STRIPS
    pairs = group_count // 2
    owned = master.shape[0]
    slots = owned * tile_count
    batch_count = lax.axis_size("batch")
    spot = lax.axis_index("batch").astype(jnp.int32).reshape(1)
    extra = extra_of(owned, batch_count)
    strips = share_out(pixels.reshape((tile_count,) + pixels.shape[3:]), "tile")
    dense = pack(master)
    paired = tile_count <= 8
    if paired:
        mine = [dense] + [swap(dense, 2 * k) for k in range(1, tile_count // 2)]
        pieces = mine + [swap(piece, 1) for piece in mine]
    else:
        pieces = [lax.all_gather(dense, "tile", axis=0, tiled=True)]

    numbers = jnp.arange(slots, dtype=jnp.int32)
    slot_of = jnp.sum(
        jnp.where(slot_owner_table[None, :] == numbers[:, None], numbers[None, :], 0), axis=1
    )
    owner = slot_of // owned
    within = slot_of - owner * owned
    place_of = within + (owned + extra) * owner
    if paired:
        apart = owner ^ tile_place
        apart = (apart & 1) * (tile_count // 2) + (apart >> 1)
        slot_of = within + owned * apart
        place_of = within + (owned + extra) * apart
    image_ids = lax.dynamic_index_in_dim(
        buckets.reshape(group_count, slot_count), tile_place, 1, keepdims=False
    )
    heights = jnp.where(image_ids == 0, 5 * CH // 9, jnp.where(image_ids == 1, 7 * CH // 9, CH))
    breadths = jnp.where(image_ids == 0, CW, jnp.where(image_ids == 1, 7 * CW // 9, 5 * CW // 9))
    sizes = jnp.stack([heights, breadths], axis=1).reshape(-1).astype(jnp.int32)

    two = 6 * C2 + HID2 + C2
    vec_two = jnp.concatenate([vectors[: 6 * C2], vectors[6 * C2 + HID2 : two]]).reshape(7, C2)
    vec_hid_two = vectors[6 * C2 : 6 * C2 + HID2].reshape(1, HID2)
    wide_end = two + 7 * C3
    vec_three = jnp.concatenate([vectors[two:wide_end], vectors[wide_end + HID3 :]])
    vec_three = jnp.pad(vec_three.reshape(8, C3), ((0, 0), (0, WIDE - C3)))
    vec_hid_three = vectors[wide_end : wide_end + HID3].reshape(1, HID3)

    goal = out_grad.reshape(pairs, 2, H3, W3, C3).transpose(0, 2, 3, 1, 4)
    goal = goal.reshape(pairs, H3, 2 * W3, C3)
    goal = jnp.pad(goal, ((0, 0), (0, 0), (0, LINE - 2 * W3), (0, WIDE - C3)))
    goal = goal.reshape(pairs, PLANE, WIDE)

    result, pixel_back, near, far = run_main(
        slot_of,
        place_of,
        sizes,
        strips,
        goal,
        (vec_two, vec_hid_two, vec_three, vec_hid_three),
        pieces,
        extra,
    )
    result = result[:, :, : 2 * W3, :C3].reshape(pairs, H3, W3, 2, C3).transpose(0, 3, 1, 2, 4)

    near = near.reshape(-1, owned + extra, HALF, 128)
    far = far.reshape(near.shape)
    if paired:
        own, *parts = fold_pair(near, swap(far, 1))
        pieces = [own] + [swap(part, 2 * k + 2) for k, part in enumerate(parts)]
    else:
        pieces = list(share_out(jnp.concatenate([near, far], axis=0), "tile"))
    own, *parts = fold_tile(spot, pieces, batch_count)
    pixel_back, own = lax.optimization_barrier((pixel_back, own))
    parts = [
        lax.ppermute(part, "batch", [(i, (i + k + 1) % batch_count) for i in range(batch_count)])
        for k, part in enumerate(parts)
    ]
    quarter, norm = fold_batch(spot, own, parts, owned, tile_count)
    quarters = [quarter] + [
        lax.ppermute(quarter, "batch", [(i, (i + k) % batch_count) for i in range(batch_count)])
        for k in range(1, batch_count)
    ]
    norm = share_out(norm, ("batch", "tile"))
    block_grad, left_new, right_new, master_new, weight_copy, whole_vector, clip = update(
        spot, norm, quarters, extra, master, left_stat, right_stat, left_root, right_root
    )
    clip_norm = clip[0, 0]
    share = vectors.shape[0] // tile_count
    whole_vector = whole_vector.reshape(-1)
    vec_grad = lax.dynamic_slice_in_dim(whole_vector, tile_place * share, share, 0)
    vec_moment = moment + vec_grad * vec_grad
    own_vectors = lax.dynamic_slice_in_dim(vectors, tile_place * share, share, 0)
    vec_new = own_vectors - rate_vector * vec_grad / (jnp.sqrt(vec_moment) + eps_adagrad)
    returned = share_out(pixel_back, "tile")
    return (
        result.reshape(out_grad.shape),
        returned.astype(f32).reshape(pixels.shape),
        clip_norm,
        block_grad,
        left_new,
        right_new,
        master_new,
        weight_copy,
        vec_grad,
        vec_moment,
        vec_new,
    )


def solution(mesh):
    placed = (
        P("batch", "tile", None, None, None, None),
        P("batch"),
        P(),
        P("batch", "tile", None, None, None, None, None),
        P("tile", None, None),
        P("tile", None, None),
        P("tile", None, None),
        P("tile", None, None),
        P("tile", None, None),
        P(),
        P("tile"),
    )
    return jax.shard_map(
        on_device,
        mesh=mesh,
        in_specs=placed,
        out_specs=(
            P("batch", "tile", None, None, None, None, None),
            P("batch", "tile", None, None, None, None),
            P(),
            P("tile", None, None),
            P("tile", None, None),
            P("tile", None, None),
            P("tile", None, None),
            P("tile", None, None),
            P("tile"),
            P("tile"),
            P("tile"),
        ),
        check_vma=False,
    )
```

```python
import functools

import jax
import jax.numpy as jnp
from jax import lax
from jax.experimental import pallas as pl
from jax.experimental.pallas import tpu as pltpu
from jax.sharding import PartitionSpec as P

C2 = 128
HID2 = 512
C3 = 320
HID3 = 1280
CH = 36
CW = 36
STRIPS = 4
BS = 64
SR = CH // STRIPS
H3 = CH // 2
W3 = CW // 2
WIDE = 384
LINE = 40
PLANE = H3 * LINE
ROWS = 6
CHUNK = ROWS * LINE
STEPS = H3 // ROWS
HALF = BS // 2

eps_norm = 1e-05
clip_limit = 1.0
rate_matrix = 0.3
rate_vector = 0.3
eps_adagrad = 1e-08
f32 = jnp.float32
bf16 = jnp.bfloat16

SHAPES = [(C2, HID2), (HID2, C2), (9 * C2, C3), (C3, HID3), (HID3, C3)]
USED = sum(rows // BS * (cols // BS) for rows, cols in SHAPES)
VEC_ROWS = (6 * C2 + HID2 + C2 + C3 + 6 * C3 + HID3 + C3) // 128


def extra_of(owned, groups):
    extra = -(-VEC_ROWS // HALF)
    return extra + -(owned + extra) % groups


def product(left, right):
    return jnp.dot(left, right, preferred_element_type=f32)


def product_nt(left, right):
    return lax.dot_general(left, right, (((1,), (1,)), ((), ())), preferred_element_type=f32)


def product_tn(left, right):
    return lax.dot_general(left, right, (((0,), (0,)), ((), ())), preferred_element_type=f32)


def gelu_pair(values):
    bell = jnp.exp2(values * values * (-0.5 * 1.4426950408889634))
    step = pl.reciprocal(1.0 + (0.3275911 * 0.7071067811865476) * jnp.abs(values), approx=True)
    tail = step * (
        0.5 * 0.254829592
        + step
        * (
            0.5 * -0.284496736
            + step
            * (0.5 * 1.421413741 + step * (0.5 * -1.453152027 + step * (0.5 * 1.061405429)))
        )
    )
    tail = tail * bell
    share = jnp.where(values >= 0.0, 1.0 - tail, tail)
    return (values * share, share + values * (bell * 0.3989422804014327))


def fold(values):
    chans = values.shape[-1]
    return jnp.sum(values.reshape(-1, 8, chans), axis=0)


def by_image(total):
    total = total + pltpu.roll(total, 4, 0)
    total = total + pltpu.roll(total, 2, 0)
    return jnp.sum(total, axis=1, keepdims=True)


def line(pattern):
    return jnp.concatenate([pattern] * (LINE // 8), axis=0)


def spread(pattern, chans):
    return line(jnp.broadcast_to(pattern, (8, chans)))


def from_left(values):
    flat = values.reshape(-1, values.shape[-1])
    return pltpu.roll(flat, 2, 0).reshape(values.shape)


def from_right(values):
    flat = values.reshape(-1, values.shape[-1])
    return pltpu.roll(flat, flat.shape[0] - 2, 0).reshape(values.shape)


def rounded(values):
    return values.astype(bf16).astype(f32)


def widen(values):
    return jnp.concatenate([values] * (WIDE // 128), axis=-1)


def norm_terms(total, square, count):
    mean = by_image(total) / count
    scaling = lax.rsqrt(by_image(square) / count - mean * mean + eps_norm)
    return (mean, scaling)


def main_kernel(
    pairs,
    strip_count,
    slots,
    extra,
    piece_count,
    slot_ref,
    place_ref,
    size_ref,
    strips_ref,
    goal_ref,
    vec_two_ref,
    vec_hid_two_ref,
    vec_three_ref,
    vec_hid_three_ref,
    *refs,
):
    inner_kernel(
        pairs,
        strip_count,
        slots,
        extra,
        slot_ref,
        place_ref,
        size_ref,
        strips_ref,
        goal_ref,
        vec_two_ref,
        vec_hid_two_ref,
        vec_three_ref,
        vec_hid_three_ref,
        refs[:piece_count],
        *refs[piece_count:],
    )


def inner_kernel(
    pairs,
    strip_count,
    slots,
    extra,
    slot_ref,
    place_ref,
    size_ref,
    strips_ref,
    goal_ref,
    vec_two_ref,
    vec_hid_two_ref,
    vec_three_ref,
    vec_hid_three_ref,
    piece_refs,
    result_ref,
    pixel_ref,
    near_ref,
    far_ref,
    gathered_ref,
    grad_ref,
    strips,
    line_tmp,
    x_ref,
    inv_ref,
    col_ref,
    pool_ref,
    mix_ref,
    zed_ref,
    dx_ref,
    u_ref,
    g_ref,
    h_ref,
    dy_ref,
    patch_ref,
    dpatch_ref,
    inv3_ref,
    e_ref,
    col3_ref,
    pool3_ref,
    mix3_ref,
    dx3_ref,
    u3_ref,
    g3_ref,
    h3_ref,
    dy3_ref,
    dpre_ref,
    w1_ref,
    w2_ref,
    we_ref,
    w3_ref,
    w4_ref,
    gw1_ref,
    gw2_ref,
    gwe_ref,
    gw3_ref,
    gw4_ref,
    acc_two,
    acc_hid_two,
    acc_three,
    acc_hid_three,
    flat_ref,
    in_sem,
    out_sem,
    piece_sem,
    grad_sem,
):
    pair = pl.program_id(0)
    weights = [w1_ref, w2_ref, we_ref, w3_ref, w4_ref]
    grads = [gw1_ref, gw2_ref, gwe_ref, gw3_ref, gw4_ref]

    def strip_copies(outward):
        copies = []
        for half in range(4):
            start = lax.rem(pair * 8 + strip_count - 2 + 2 * half, strip_count)
            inside = strips.at[pl.ds(2 * half, 2)]
            if outward:
                copies.append(
                    pltpu.make_async_copy(inside, pixel_ref.at[pl.ds(start, 2)], out_sem.at[half])
                )
            else:
                copies.append(
                    pltpu.make_async_copy(strips_ref.at[pl.ds(start, 2)], inside, in_sem.at[half])
                )
        return copies

    for copy in strip_copies(False):
        copy.start()

    left_half = lax.broadcasted_iota(jnp.int32, (HALF, 128), 1) < BS

    def piece_copies():
        count = slots // len(piece_refs)
        return [
            pltpu.make_async_copy(
                ref, gathered_ref.at[pl.ds(n * count, count)], piece_sem.at[n]
            )
            for n, ref in enumerate(piece_refs)
        ]

    def grad_copies():
        half = grad_ref.shape[0] // 2
        return [
            pltpu.make_async_copy(grad_ref.at[pl.ds(n * half, half)], ref, grad_sem.at[n])
            for n, ref in enumerate((near_ref, far_ref))
        ]

    def unpack():
        for copy in piece_copies():
            copy.wait()
        offset = 0
        for (rows, cols), ref in zip(SHAPES, weights):
            wide = cols // BS
            for rb in range(rows // BS):
                for cb in range(0, wide, 2):
                    number = offset + rb * wide + cb
                    first = gathered_ref[slot_ref[number]].astype(f32)
                    turned = pltpu.roll(first, BS, 1)
                    if cb + 1 < wide:
                        second = gathered_ref[slot_ref[number + 1]].astype(f32)
                        top = jnp.where(left_half, first, pltpu.roll(second, BS, 1))
                        low = jnp.where(left_half, turned, second)
                    else:
                        top = jnp.where(left_half, first, 0.0)
                        low = jnp.where(left_half, turned, 0.0)
                    place = slice(cb * BS, cb * BS + 128)
                    ref[rb * BS : rb * BS + HALF, place] = top.astype(bf16)
                    ref[rb * BS + HALF : rb * BS + BS, place] = low.astype(bf16)
            offset += rows // BS * wide
        w3_ref[C3:, :] = jnp.zeros((WIDE - C3, HID3), bf16)

    @pl.when(pair == 0)
    def _():
        for copy in piece_copies():
            copy.start()
        unpack()
        acc_two[...] = jnp.zeros(acc_two.shape, f32)
        acc_hid_two[...] = jnp.zeros(acc_hid_two.shape, f32)
        acc_three[...] = jnp.zeros(acc_three.shape, f32)
        acc_hid_three[...] = jnp.zeros(acc_hid_three.shape, f32)

    parity = lax.broadcasted_iota(jnp.int32, (8, 128), 0) % 2
    high = jnp.where(parity == 0, size_ref[pair * 4], size_ref[pair * 4 + 2])
    broad = jnp.where(parity == 0, size_ref[pair * 4 + 1], size_ref[pair * 4 + 3])
    count_two = (high * broad * C2).astype(f32)[:, :1]
    high3 = (high + 1) // 2
    broad3 = (broad + 1) // 2
    count_three = (high3 * broad3 * C3).astype(f32)[:, :1]
    place = lax.broadcasted_iota(jnp.int32, (LINE, 128), 0) // 2
    inside = lax.broadcasted_iota(jnp.int32, (LINE, 128), 0) < 2 * W3
    reach = []
    col_share = []
    for pc in range(2):
        column = 2 * place + pc
        reach.append(jnp.where(inside & (column < line(broad)), line(high), 0))
        edge = (column == 0) | (column == line(broad) - 1)
        col_share.append(jnp.where(edge, 0.5, 1.0 / 3.0))
    reach3 = jnp.where(inside & (place < line(broad3)), line(high3), 0)
    edge3 = (place == 0) | (place == line(broad3) - 1)
    col_share3 = jnp.where(edge3, 0.5, 1.0 / 3.0)

    def row_share(row, height):
        return jnp.where((row == 0) | (row == height - 1), 0.5, 1.0 / 3.0)

    gain1, bias1, scale1 = (vec_two_ref[n : n + 1] for n in range(3))
    gain2, bias2, scale2, out_bias = (vec_two_ref[n : n + 1] for n in range(3, 7))
    embed_bias, gain3, bias3, scale3 = (vec_three_ref[n : n + 1] for n in range(4))
    gain4, bias4, scale4, out_bias3 = (vec_three_ref[n : n + 1] for n in range(4, 8))

    for copy in strip_copies(False):
        copy.wait()

    zero_line = jnp.zeros((1, LINE, C2), f32)
    zero_line3 = jnp.zeros((1, LINE, WIDE), f32)
    for plane in range(4):
        col_ref[plane, 0:1] = zero_line
        col_ref[plane, H3 + 1 : H3 + 2] = zero_line
        zed_ref[plane, 0:1] = zero_line
    col3_ref[0:1] = zero_line3
    col3_ref[H3 + 1 : H3 + 2] = zero_line3

    def arrange(r, carry):
        total, square = carry
        for pr in range(2):
            row = 2 * r + pr
            strip = row // SR
            within = row - strip * SR
            for image in range(2):
                spot = pr * 2 + image
                line_tmp[spot, 0:CW] = strips[image * STRIPS + strip, within].astype(f32)
                for pc in range(2):
                    x_ref[pr * 2 + pc, r, pl.ds(image, W3, stride=2)] = line_tmp[
                        spot, pl.ds(pc, W3, stride=2)
                    ]
            for pc in range(2):
                plane = pr * 2 + pc
                valid = row < reach[pc]
                inv_ref[plane, r] = jnp.where(
                    valid, line(row_share(row, high)) * col_share[pc], 0.0
                )
                values = jnp.where(valid, x_ref[plane, r], 0.0)
                x_ref[plane, r] = values
                total = total + fold(values)
                square = square + fold(values * values)
        inv3_ref[r] = jnp.where(r < reach3, line(row_share(r, high3)) * col_share3, 0.0)
        return (total, square)

    nothing = jnp.zeros((8, C2), f32)
    nothing3 = jnp.zeros((8, WIDE), f32)
    total, square = lax.fori_loop(0, H3, arrange, (nothing, nothing))
    mean1, scaling1 = norm_terms(total, square, count_two)
    factor1 = line(scaling1 * gain1)
    shift1 = line(bias1 - mean1 * scaling1 * gain1)

    def window_cols(k, carry):
        rows = pl.ds(2 * k, 2)
        for pr in range(2):
            masked = []
            for pc in range(2):
                plane = pr * 2 + pc
                normal = rounded(x_ref[plane, rows] * factor1 + shift1)
                masked.append(jnp.where(inv_ref[plane, rows] > 0.0, normal, 0.0))
            both = masked[0] + masked[1]
            col_ref[pr * 2, pl.ds(2 * k + 1, 2)] = both + from_left(masked[1])
            col_ref[pr * 2 + 1, pl.ds(2 * k + 1, 2)] = both + from_right(masked[0])
        return carry

    lax.fori_loop(0, H3 // 2, window_cols, 0)

    def row_windows(pc, k):
        even = col_ref[pc, pl.ds(2 * k + 1, 2)]
        odd = col_ref[2 + pc, pl.ds(2 * k + 1, 2)]
        both = even + odd
        return (both + col_ref[2 + pc, pl.ds(2 * k, 2)], both + col_ref[pc, pl.ds(2 * k + 2, 2)])

    def mix(k, carry):
        total, square = carry
        rows = pl.ds(2 * k, 2)
        for pc in range(2):
            windows = row_windows(pc, k)
            for pr in range(2):
                plane = pr * 2 + pc
                values = x_ref[plane, rows]
                share = inv_ref[plane, rows]
                pooled = windows[pr] * share - rounded(values * factor1 + shift1)
                pooled = jnp.where(share > 0.0, pooled, 0.0)
                mixed = values + scale1 * pooled
                pool_ref[plane, rows] = pooled
                mix_ref[plane, rows] = mixed
                total = total + fold(mixed)
                square = square + fold(mixed * mixed)
        return (total, square)

    total, square = lax.fori_loop(0, H3 // 2, mix, (nothing, nothing))
    mean2, scaling2 = norm_terms(total, square, count_two)
    factor2 = line(scaling2 * gain2)
    shift2 = line(bias2 - mean2 * scaling2 * gain2)

    def where_chunk(c):
        plane = c // STEPS
        first = (c - plane * STEPS) * ROWS
        return (plane, first, pl.ds(pl.multiple_of(c * CHUNK, CHUNK), CHUNK))

    def branch(c, carry):
        plane, first, flat = where_chunk(c)
        mixed = mix_ref[plane, pl.ds(first, ROWS)]
        low = (mixed * factor2 + shift2).reshape(CHUNK, C2).astype(bf16)
        h_ref[flat] = low
        hidden = product(low, w1_ref[...]) + vec_hid_two_ref[...]
        active, slope = gelu_pair(hidden)
        active = active.astype(bf16)
        u_ref[flat] = active
        g_ref[flat] = slope.astype(bf16)
        out = (product(active, w2_ref[...]) + out_bias).reshape(ROWS, LINE, C2)
        valid = inv_ref[plane, pl.ds(first, ROWS)] > 0.0
        zed = rounded(jnp.where(valid, mixed + scale2 * out, 0.0))
        zed_ref[plane, pl.ds(first + 1, ROWS)] = zed
        return carry

    lax.fori_loop(0, 4 * STEPS, branch, 0)

    def patches(k, carry):
        flat = pl.ds(pl.multiple_of(k * 2 * LINE, 2 * LINE), 2 * LINE)
        for ky in range(3):
            pr = (0 if ky == 1 else 1) * 2
            rows = pl.ds(2 * k + (0 if ky == 0 else 1), 2)
            even = zed_ref[pr, rows]
            odd = zed_ref[pr + 1, rows]
            for kx, tap in enumerate((from_left(odd), even, odd)):
                at = (3 * ky + kx) * C2
                patch_ref[flat, at : at + C2] = tap.reshape(2 * LINE, C2).astype(bf16)
        return carry

    lax.fori_loop(0, H3 // 2, patches, 0)

    def embed(c, carry):
        total, square = carry
        flat = pl.ds(pl.multiple_of(c * CHUNK, CHUNK), CHUNK)
        rows = pl.ds(c * ROWS, ROWS)
        out = (product(patch_ref[flat], we_ref[...]) + embed_bias).reshape(ROWS, LINE, WIDE)
        out = jnp.where(widen(inv3_ref[rows]) > 0.0, out, 0.0)
        e_ref[rows] = out
        return (total + fold(out), square + fold(out * out))

    total, square = lax.fori_loop(0, STEPS, embed, (nothing3, nothing3))
    mean3, scaling3 = norm_terms(total, square, count_three)
    factor3 = line(scaling3 * gain3)
    shift3 = line(bias3 - mean3 * scaling3 * gain3)

    def window_cols3(k, carry):
        rows = pl.ds(2 * k, 2)
        normal = rounded(e_ref[rows] * factor3 + shift3)
        masked = jnp.where(widen(inv3_ref[rows]) > 0.0, normal, 0.0)
        col3_ref[pl.ds(2 * k + 1, 2)] = masked + from_left(masked) + from_right(masked)
        return carry

    lax.fori_loop(0, H3 // 2, window_cols3, 0)

    def row_windows3(k):
        return (
            col3_ref[pl.ds(2 * k, 2)]
            + col3_ref[pl.ds(2 * k + 1, 2)]
            + col3_ref[pl.ds(2 * k + 2, 2)]
        )

    def mix3(k, carry):
        total, square = carry
        rows = pl.ds(2 * k, 2)
        values = e_ref[rows]
        share = widen(inv3_ref[rows])
        pooled = row_windows3(k) * share - rounded(values * factor3 + shift3)
        pooled = jnp.where(share > 0.0, pooled, 0.0)
        mixed = values + scale3 * pooled
        pool3_ref[rows] = pooled
        mix3_ref[rows] = mixed
        return (total + fold(mixed), square + fold(mixed * mixed))

    total, square = lax.fori_loop(0, H3 // 2, mix3, (nothing3, nothing3))
    mean4, scaling4 = norm_terms(total, square, count_three)
    factor4 = line(scaling4 * gain4)
    shift4 = line(bias4 - mean4 * scaling4 * gain4)
    normal4 = (spread(scaling4, WIDE), spread(-mean4 * scaling4, WIDE))

    def branch3(c, carry):
        d_out_bias, d_scale, d_hidden_bias, d_shift, d_gain = carry
        flat = pl.ds(pl.multiple_of(c * CHUNK, CHUNK), CHUNK)
        rows = pl.ds(c * ROWS, ROWS)
        mixed = mix3_ref[rows]
        low = (mixed * factor4 + shift4).reshape(CHUNK, WIDE).astype(bf16)
        h3_ref[flat] = low
        hidden = product(low, w3_ref[...]) + vec_hid_three_ref[...]
        active, slope = gelu_pair(hidden)
        active = active.astype(bf16)
        u3_ref[flat] = active
        out = (product(active, w4_ref[...]) + out_bias3).reshape(ROWS, LINE, WIDE)
        valid = widen(inv3_ref[rows]) > 0.0
        out = jnp.where(valid, out, 0.0)
        result_ref[0, rows] = mixed + scale4 * out
        goal = jnp.where(valid, goal_ref[0, flat].astype(f32).reshape(ROWS, LINE, WIDE), 0.0)
        low_goal = (scale4 * goal).reshape(CHUNK, WIDE).astype(bf16)
        dy3_ref[flat] = low_goal
        d_hidden = (slope * product_nt(low_goal, w4_ref[...])).astype(bf16)
        g3_ref[flat] = d_hidden
        d_low = product_nt(d_hidden, w3_ref[...]).reshape(ROWS, LINE, WIDE)
        dx3_ref[rows] = d_low
        normal = mixed * normal4[0] + normal4[1]
        return (
            d_out_bias + fold(low_goal.astype(f32)),
            d_scale + fold(out * goal),
            d_hidden_bias + fold(d_hidden.astype(f32)),
            d_shift + fold(d_low),
            d_gain + fold(d_low * normal),
        )

    wide_zero = jnp.zeros((8, HID3), f32)
    d_out_bias, d_scale, d_hidden_bias, d_shift, d_gain = lax.fori_loop(
        0, STEPS, branch3, (nothing3, nothing3, wide_zero, nothing3, nothing3)
    )
    acc_three[7] += d_out_bias
    acc_three[6] += d_scale
    acc_hid_three[...] += d_hidden_bias
    acc_three[5] += d_shift
    acc_three[4] += d_gain
    mean_shift = by_image(d_shift * gain4) / count_three
    mean_gain = by_image(d_gain * gain4) / count_three

    def keep(ref, value):
        if pairs == 1:
            ref[...] = value
        else:

            @pl.when(pair == 0)
            def _():
                ref[...] = value

            @pl.when(pair > 0)
            def _():
                ref[...] += value

    keep(gw3_ref, product_tn(h3_ref[...], g3_ref[...]))
    keep(gw4_ref, product_tn(u3_ref[...], dy3_ref[...]))

    back_gain4 = line(scaling4 * gain4)
    back_mean4 = spread(scaling4 * mean_shift, WIDE)
    back_normal4 = spread(scaling4 * mean_gain, WIDE)

    def unmix3(k, d_scale):
        rows = pl.ds(2 * k, 2)
        flat = pl.ds(pl.multiple_of(k * 2 * LINE, 2 * LINE), 2 * LINE)
        share = widen(inv3_ref[rows])
        valid = share > 0.0
        normal = mix3_ref[rows] * normal4[0] + normal4[1]
        back = dx3_ref[rows] * back_gain4 - back_mean4 - normal * back_normal4
        goal = goal_ref[0, flat].astype(f32).reshape(2, LINE, WIDE)
        d_mixed = jnp.where(valid, back + goal, 0.0)
        dx3_ref[rows] = d_mixed
        d_scale = d_scale + fold(pool3_ref[rows] * d_mixed)
        weighted = scale3 * d_mixed * share
        col3_ref[pl.ds(2 * k + 1, 2)] = weighted + from_left(weighted) + from_right(weighted)
        return d_scale

    acc_three[3] += lax.fori_loop(0, H3 // 2, unmix3, nothing3)
    normal3 = (spread(scaling3, WIDE), spread(-mean3 * scaling3, WIDE))

    def unpool3(k, carry):
        d_shift, d_gain = carry
        rows = pl.ds(2 * k, 2)
        valid = widen(inv3_ref[rows]) > 0.0
        d_normal = jnp.where(valid, row_windows3(k) - scale3 * dx3_ref[rows], 0.0)
        pool3_ref[rows] = d_normal
        normal = e_ref[rows] * normal3[0] + normal3[1]
        return (d_shift + fold(d_normal), d_gain + fold(d_normal * normal))

    d_shift, d_gain = lax.fori_loop(0, H3 // 2, unpool3, (nothing3, nothing3))
    acc_three[2] += d_shift
    acc_three[1] += d_gain
    mean_shift = by_image(d_shift * gain3) / count_three
    mean_gain = by_image(d_gain * gain3) / count_three
    back_gain3 = line(scaling3 * gain3)
    back_mean3 = spread(scaling3 * mean_shift, WIDE)
    back_normal3 = spread(scaling3 * mean_gain, WIDE)

    def unnorm3(k, d_bias):
        rows = pl.ds(2 * k, 2)
        flat = pl.ds(pl.multiple_of(k * 2 * LINE, 2 * LINE), 2 * LINE)
        valid = widen(inv3_ref[rows]) > 0.0
        normal = e_ref[rows] * normal3[0] + normal3[1]
        back = pool3_ref[rows] * back_gain3 - back_mean3 - normal * back_normal3
        low = jnp.where(valid, dx3_ref[rows] + back, 0.0).astype(bf16)
        dpre_ref[flat] = low.reshape(2 * LINE, WIDE)
        return d_bias + fold(low.astype(f32))

    acc_three[0] += lax.fori_loop(0, H3 // 2, unnorm3, nothing3)
    keep(gwe_ref, product_tn(patch_ref[...], dpre_ref[...]))

    def unpatch(c, carry):
        flat = pl.ds(pl.multiple_of(c * CHUNK, CHUNK), CHUNK)
        rows = pl.ds(c * ROWS, ROWS)
        dpatch_ref[rows] = product_nt(dpre_ref[flat], we_ref[...]).reshape(ROWS, LINE, 9 * C2)
        return carry

    lax.fori_loop(0, STEPS, unpatch, 0)
    dpatch_ref[H3 : H3 + 1] = jnp.zeros((1, LINE, 9 * C2), f32)

    def tap(ky, kx, rows):
        at = (3 * ky + kx) * C2
        return dpatch_ref[rows, :, at : at + C2]

    def gather_back(k, carry):
        here = pl.ds(2 * k, 2)
        below = pl.ds(2 * k + 1, 2)
        sources = []
        for ky, rows in ((0, below), (1, here), (2, here)):
            sources.append((tap(ky, 1, rows), tap(ky, 2, rows) + from_right(tap(ky, 0, rows))))
        for pc in range(2):
            for pr, value in ((0, sources[1][pc]), (1, sources[2][pc] + sources[0][pc])):
                plane = pr * 2 + pc
                valid = inv_ref[plane, here] > 0.0
                zed_ref[plane, here] = jnp.where(valid, rounded(value), 0.0)
        return carry

    lax.fori_loop(0, H3 // 2, gather_back, 0)

    normal2 = (spread(scaling2, C2), spread(-mean2 * scaling2, C2))

    def unbranch(c, carry):
        d_out_bias, d_hidden_bias, d_shift, d_gain = carry
        plane, first, flat = where_chunk(c)
        rows = pl.ds(first, ROWS)
        low_goal = (scale2 * zed_ref[plane, rows]).reshape(CHUNK, C2).astype(bf16)
        dy_ref[flat] = low_goal
        d_hidden = g_ref[flat].astype(f32) * product_nt(low_goal, w2_ref[...])
        d_hidden = d_hidden.astype(bf16)
        g_ref[flat] = d_hidden
        d_low = product_nt(d_hidden, w1_ref[...]).reshape(ROWS, LINE, C2)
        dx_ref[plane, rows] = d_low
        normal = mix_ref[plane, rows] * normal2[0] + normal2[1]
        return (
            d_out_bias + fold(low_goal.astype(f32)),
            d_hidden_bias + fold(d_hidden.astype(f32)),
            d_shift + fold(d_low),
            d_gain + fold(d_low * normal),
        )

    d_out_bias, d_hidden_bias, d_shift, d_gain = lax.fori_loop(
        0, 4 * STEPS, unbranch, (nothing, jnp.zeros((8, HID2), f32), nothing, nothing)
    )
    acc_two[6] += d_out_bias
    acc_hid_two[...] += d_hidden_bias
    acc_two[4] += d_shift
    acc_two[3] += d_gain
    mean_shift = by_image(d_shift * gain2) / count_two
    mean_gain = by_image(d_gain * gain2) / count_two
    keep(gw1_ref, product_tn(h_ref[...], g_ref[...]))
    new_gw2 = product_tn(dy_ref[...], u_ref[...]).T
    keep(gw2_ref, new_gw2)
    d_scale = fold(w2_ref[...].astype(f32) * new_gw2) + out_bias * d_out_bias
    acc_two[5] += d_scale / scale2

    back_gain2 = line(scaling2 * gain2)
    back_mean2 = spread(scaling2 * mean_shift, C2)
    back_normal2 = spread(scaling2 * mean_gain, C2)

    def unmix(k, d_scale):
        rows = pl.ds(2 * k, 2)
        for pr in range(2):
            weighted = []
            for pc in range(2):
                plane = pr * 2 + pc
                share = inv_ref[plane, rows]
                normal = mix_ref[plane, rows] * normal2[0] + normal2[1]
                back = dx_ref[plane, rows] * back_gain2 - back_mean2 - normal * back_normal2
                d_mixed = jnp.where(share > 0.0, zed_ref[plane, rows] + back, 0.0)
                dx_ref[plane, rows] = d_mixed
                d_scale = d_scale + fold(pool_ref[plane, rows] * d_mixed)
                weighted.append(scale1 * d_mixed * share)
            both = weighted[0] + weighted[1]
            col_ref[pr * 2, pl.ds(2 * k + 1, 2)] = both + from_left(weighted[1])
            col_ref[pr * 2 + 1, pl.ds(2 * k + 1, 2)] = both + from_right(weighted[0])
        return d_scale

    acc_two[2] += lax.fori_loop(0, H3 // 2, unmix, nothing)
    normal1 = (spread(scaling1, C2), spread(-mean1 * scaling1, C2))

    def unpool(k, carry):
        d_shift, d_gain = carry
        rows = pl.ds(2 * k, 2)
        for pc in range(2):
            windows = row_windows(pc, k)
            for pr in range(2):
                plane = pr * 2 + pc
                valid = inv_ref[plane, rows] > 0.0
                d_normal = windows[pr] - scale1 * dx_ref[plane, rows]
                d_normal = jnp.where(valid, d_normal, 0.0)
                pool_ref[plane, rows] = d_normal
                normal = x_ref[plane, rows] * normal1[0] + normal1[1]
                d_shift = d_shift + fold(d_normal)
                d_gain = d_gain + fold(d_normal * normal)
        return (d_shift, d_gain)

    d_shift, d_gain = lax.fori_loop(0, H3 // 2, unpool, (nothing, nothing))
    acc_two[1] += d_shift
    acc_two[0] += d_gain
    mean_shift = by_image(d_shift * gain1) / count_two
    mean_gain = by_image(d_gain * gain1) / count_two
    back_gain1 = line(scaling1 * gain1)
    back_mean1 = spread(scaling1 * mean_shift, C2)
    back_normal1 = spread(scaling1 * mean_gain, C2)

    def unnorm(r, carry):
        for pr in range(2):
            row = 2 * r + pr
            strip = row // SR
            within = row - strip * SR
            for pc in range(2):
                plane = pr * 2 + pc
                normal = x_ref[plane, r] * normal1[0] + normal1[1]
                back = pool_ref[plane, r] * back_gain1 - back_mean1 - normal * back_normal1
                dx_ref[plane, r] = jnp.where(
                    inv_ref[plane, r] > 0.0, dx_ref[plane, r] + back, 0.0
                )
            for image in range(2):
                spot = pr * 2 + image
                for pc in range(2):
                    line_tmp[spot, pl.ds(pc, W3, stride=2)] = dx_ref[
                        pr * 2 + pc, r, pl.ds(image, W3, stride=2)
                    ]
                strips[image * STRIPS + strip, within] = line_tmp[spot, 0:CW].astype(bf16)
        return carry

    lax.fori_loop(0, H3, unnorm, 0)
    for copy in strip_copies(True):
        copy.start()

    @pl.when(pair == pairs - 1)
    def _():
        offset = 0
        for (rows, cols), ref in zip(SHAPES, grads):
            wide = cols // BS
            for rb in range(rows // BS):
                for cb in range(0, wide, 2):
                    number = offset + rb * wide + cb
                    at = slice(cb * BS, cb * BS + 128)
                    top = ref[rb * BS : rb * BS + HALF, at]
                    low = ref[rb * BS + HALF : rb * BS + BS, at]
                    grad_ref[place_ref[number]] = jnp.where(
                        left_half, top, pltpu.roll(low, BS, 1)
                    ).astype(bf16)
                    if cb + 1 < wide:
                        grad_ref[place_ref[number + 1]] = jnp.where(
                            left_half, pltpu.roll(top, BS, 1), low
                        ).astype(bf16)
            offset += rows // BS * wide

        def filler(number, carry):
            grad_ref[place_ref[number]] = jnp.zeros((HALF, 128), bf16)
            return carry

        lax.fori_loop(USED, slots, filler, 0)

        flat_ref[...] = jnp.zeros(flat_ref.shape, f32)

        def put(at, total, length):
            if at % 128:
                room = jnp.zeros((8, 128), f32)
                if total.shape[1] < length + BS:
                    total = jnp.concatenate([total, room], axis=1)
                total = pltpu.roll(total, BS, 1)
            whole = jnp.sum(total, axis=0, keepdims=True)
            done = -(at % 128)
            row = at // 128
            lane = 0
            while done < length:
                first = max(0, -done)
                last = min(128, length - done)
                flat_ref[row : row + 1, first:last] = whole[:, lane + first : lane + last]
                done += 128
                lane += 128
                row += 1

        at = 0
        for n in range(6):
            put(at, acc_two[n], C2)
            at += C2
        put(at, acc_hid_two[...], HID2)
        at += HID2
        put(at, acc_two[6], C2)
        at += C2
        for n in range(7):
            put(at, acc_three[n], C3)
            at += C3
        put(at, acc_hid_three[...], HID3)
        at += HID3
        put(at, acc_three[7], C3)
        packed = flat_ref[...].astype(bf16)
        stride = slots // strip_count + extra
        for n in range(extra):
            piece = packed[n * HALF : (n + 1) * HALF]

            def leave(target, carry):
                grad_ref[target * stride + stride - extra + n] = piece
                return carry

            lax.fori_loop(0, strip_count, leave, 0)
        for copy in grad_copies():
            copy.start()
        for copy in grad_copies():
            copy.wait()

    for copy in strip_copies(True):
        copy.wait()


def run_main(slot_of, place_of, sizes, strips, goal, vectors, pieces, extra):
    strip_count = strips.shape[0]
    pairs = goal.shape[0]
    slots = sum(piece.shape[0] for piece in pieces)
    rows_out = slots + extra * strip_count

    def whole(shape):
        return pl.BlockSpec(shape, lambda t: (0,) * len(shape), pipeline_mode=pl.Buffered(1))

    smem = pl.BlockSpec(memory_space=pltpu.SMEM)
    anywhere = pl.BlockSpec(memory_space=pl.ANY)
    plane_f32 = pltpu.VMEM((4, H3, LINE, C2), f32)
    wide_f32 = pltpu.VMEM((H3, LINE, WIDE), f32)
    scratch = [
        pltpu.VMEM((slots, HALF, 128), bf16),
        pltpu.VMEM((rows_out, HALF, 128), bf16),
        pltpu.VMEM((2 * STRIPS, SR, CW, C2), bf16),
        pltpu.VMEM((4, LINE, C2), f32),
        plane_f32,
        plane_f32,
        pltpu.VMEM((4, H3 + 2, LINE, C2), f32),
        plane_f32,
        plane_f32,
        pltpu.VMEM((4, H3 + 1, LINE, C2), f32),
        plane_f32,
        pltpu.VMEM((4 * PLANE, HID2), bf16),
        pltpu.VMEM((4 * PLANE, HID2), bf16),
        pltpu.VMEM((4 * PLANE, C2), bf16),
        pltpu.VMEM((4 * PLANE, C2), bf16),
        pltpu.VMEM((PLANE, 9 * C2), bf16),
        pltpu.VMEM((H3 + 1, LINE, 9 * C2), f32),
        pltpu.VMEM((H3, LINE, 128), f32),
        wide_f32,
        pltpu.VMEM((H3 + 2, LINE, WIDE), f32),
        wide_f32,
        wide_f32,
        wide_f32,
        pltpu.VMEM((PLANE, HID3), bf16),
        pltpu.VMEM((PLANE, HID3), bf16),
        pltpu.VMEM((PLANE, WIDE), bf16),
        pltpu.VMEM((PLANE, WIDE), bf16),
        pltpu.VMEM((PLANE, WIDE), bf16),
        pltpu.VMEM((C2, HID2), bf16),
        pltpu.VMEM((HID2, C2), bf16),
        pltpu.VMEM((9 * C2, WIDE), bf16),
        pltpu.VMEM((WIDE, HID3), bf16),
        pltpu.VMEM((HID3, WIDE), bf16),
        pltpu.VMEM((C2, HID2), f32),
        pltpu.VMEM((HID2, C2), f32),
        pltpu.VMEM((9 * C2, WIDE), f32),
        pltpu.VMEM((WIDE, HID3), f32),
        pltpu.VMEM((HID3, WIDE), f32),
        pltpu.VMEM((7, 8, C2), f32),
        pltpu.VMEM((8, HID2), f32),
        pltpu.VMEM((8, 8, WIDE), f32),
        pltpu.VMEM((8, HID3), f32),
        pltpu.VMEM((extra * HALF, 128), f32),
        pltpu.SemaphoreType.DMA((4,)),
        pltpu.SemaphoreType.DMA((4,)),
        pltpu.SemaphoreType.DMA((len(pieces),)),
        pltpu.SemaphoreType.DMA((2,)),
    ]
    return pl.pallas_call(
        functools.partial(main_kernel, pairs, strip_count, slots, extra, len(pieces)),
        grid=(pairs,),
        in_specs=[
            smem,
            smem,
            smem,
            anywhere,
            pl.BlockSpec((1,) + goal.shape[1:], lambda t: (t, 0, 0)),
        ]
        + [whole(vector.shape) for vector in vectors]
        + [anywhere] * len(pieces),
        out_specs=[
            pl.BlockSpec((1, H3, LINE, WIDE), lambda t: (t, 0, 0, 0)),
            anywhere,
            anywhere,
            anywhere,
        ],
        out_shape=[
            jax.ShapeDtypeStruct((pairs, H3, LINE, WIDE), f32),
            jax.ShapeDtypeStruct(strips.shape, bf16),
            jax.ShapeDtypeStruct((rows_out // 2, HALF, 128), bf16),
            jax.ShapeDtypeStruct((rows_out // 2, HALF, 128), bf16),
        ],
        scratch_shapes=scratch,
        compiler_params=pltpu.CompilerParams(vmem_limit_bytes=62 * 1024 * 1024),
        name="blocks",
    )(slot_of, place_of, sizes, strips, goal, *vectors, *pieces)


def pack_kernel(master_ref, dense_ref):
    values = master_ref[...]
    dense_ref[...] = jnp.concatenate([values[:, :HALF], values[:, HALF:]], axis=2).astype(bf16)


def pack(master):
    owned = master.shape[0]
    return pl.pallas_call(
        pack_kernel,
        out_shape=jax.ShapeDtypeStruct((owned, HALF, 2 * BS), bf16),
        name="pack",
    )(master)


def fold_pair_kernel(near_ref, got_ref, own_ref, *part_refs):
    for n in range(len(part_refs) + 1):
        total = near_ref[n].astype(f32) + got_ref[n].astype(f32)
        if n == 0:
            own_ref[...] = total
        else:
            part_refs[n - 1][...] = total.astype(bf16)


def fold_pair(near, got):
    part = jax.ShapeDtypeStruct(near.shape[1:], bf16)
    own = jax.ShapeDtypeStruct(near.shape[1:], f32)
    return pl.pallas_call(
        fold_pair_kernel,
        out_shape=[own] + [part] * (near.shape[0] - 1),
        name="fold_pair",
    )(near, got)


def fold_tile_kernel(pieces, spot_ref, *refs):
    piece_refs, (own_ref, *part_refs) = refs[:pieces], refs[pieces:]
    groups = len(part_refs) + 1
    share = own_ref.shape[0]
    for k in range(groups):
        start = lax.rem(spot_ref[0] + k, groups) * share
        total = piece_refs[0][pl.ds(start, share)].astype(f32)
        for ref in piece_refs[1:]:
            total = total + ref[pl.ds(start, share)].astype(f32)
        if k == 0:
            own_ref[...] = total
        else:
            part_refs[k - 1][...] = total.astype(bf16)


def fold_tile(spot, pieces, groups):
    share = pieces[0].shape[0] // groups
    part = jax.ShapeDtypeStruct((share,) + pieces[0].shape[1:], bf16)
    own = jax.ShapeDtypeStruct(part.shape, f32)
    return pl.pallas_call(
        functools.partial(fold_tile_kernel, len(pieces)),
        in_specs=[pl.BlockSpec(memory_space=pltpu.SMEM)]
        + [pl.BlockSpec(memory_space=pltpu.VMEM)] * len(pieces),
        out_shape=[own] + [part] * (groups - 1),
        name="fold_tile",
    )(spot, *pieces)


def fold_batch_kernel(owned, vector_weight, spot_ref, own_ref, *refs):
    part_refs, (total_ref, norm_ref) = refs[:-2], refs[-2:]
    share = own_ref.shape[0]
    square = jnp.zeros((8, 128), f32)
    for n in range(share):
        total = own_ref[n]
        for ref in part_refs:
            total = total + ref[n].astype(f32)
        total_ref[n] = total.astype(bf16)
        weight = jnp.where(spot_ref[0] * share + n < owned, 1.0, vector_weight)
        square = square + weight * fold(total * total)
    square = jnp.sum(jnp.sum(square, axis=1, keepdims=True), axis=0, keepdims=True)
    norm_ref[...] = jnp.broadcast_to(square[None], norm_ref.shape)


def fold_batch(spot, own, parts, owned, tile_count):
    count = tile_count * (len(parts) + 1)
    vmem = pl.BlockSpec(memory_space=pltpu.VMEM)
    return pl.pallas_call(
        functools.partial(fold_batch_kernel, owned, 1.0 / tile_count),
        in_specs=[pl.BlockSpec(memory_space=pltpu.SMEM)] + [vmem] * (len(parts) + 1),
        out_shape=[
            jax.ShapeDtypeStruct(own.shape, bf16),
            jax.ShapeDtypeStruct((count, 1, 128), f32),
        ],
        name="fold_batch",
    )(spot, own, *parts)


def update_kernel(owned, groups, spot_ref, norm_ref, *refs):
    quarters = refs[:groups]
    (
        master_ref,
        left_stat_ref,
        right_stat_ref,
        left_root_ref,
        right_root_ref,
        grad_ref,
        left_ref,
        right_ref,
        new_ref,
        copy_ref,
        vector_ref,
        clip_ref,
    ) = refs[groups:]
    share = quarters[0].shape[0]
    part = grad_ref.shape[0]
    step = pl.program_id(0)
    norm = jnp.sqrt(jnp.sum(norm_ref[...], axis=0))
    factor = jnp.minimum(1.0, clip_limit / norm)

    def summed(number):
        source = number // share
        local = number - source * share
        turn = lax.rem(spot_ref[0] - source + groups, groups)
        value = quarters[0][local].astype(f32)
        for k in range(1, groups):
            value = jnp.where(turn == k, quarters[k][local].astype(f32), value)
        return value * factor

    @pl.when(step == 0)
    def _():
        clip_ref[...] = norm
        for n in range(vector_ref.shape[0]):
            vector_ref[n] = summed(owned + n)

    for n in range(part):
        dense = summed(jnp.minimum(step * part + n, owned - 1))
        grad = jnp.concatenate([dense[:, :BS], dense[:, BS:]], axis=0)
        grad_ref[n] = grad
        low = grad.astype(bf16)
        left_ref[n] = 0.5 * left_stat_ref[n] + 0.5 * product_nt(low, low)
        right_ref[n] = 0.5 * right_stat_ref[n] + 0.5 * product_tn(low, low)
        stepped = product(left_root_ref[n].astype(bf16), low).astype(bf16)
        stepped = product(stepped, right_root_ref[n].astype(bf16))
        new = master_ref[n] - rate_matrix * stepped
        new_ref[n] = new
        copy_ref[n] = new.astype(bf16)


def update(spot, norm, quarters, extra, master, *stats):
    owned = master.shape[0]
    part = min(owned, 7)
    groups = len(quarters)
    square = pl.BlockSpec((part, BS, BS), lambda t: (t, 0, 0))
    shape = jax.ShapeDtypeStruct(master.shape, f32)

    def whole(shape):
        return pl.BlockSpec(shape, lambda t: (0,) * len(shape))

    return pl.pallas_call(
        functools.partial(update_kernel, owned, groups),
        grid=(-(-owned // part),),
        in_specs=[pl.BlockSpec(memory_space=pltpu.SMEM), whole(norm.shape)]
        + [whole(quarters[0].shape)] * groups
        + [square] * 5,
        out_specs=[square] * 5 + [whole((extra, HALF, 128)), whole((1, 128))],
        out_shape=[shape] * 4
        + [
            jax.ShapeDtypeStruct(master.shape, bf16),
            jax.ShapeDtypeStruct((extra, HALF, 128), f32),
            jax.ShapeDtypeStruct((1, 128), f32),
        ],
        compiler_params=pltpu.CompilerParams(vmem_limit_bytes=32 * 1024 * 1024),
        name="update",
    )(spot, norm, *quarters, master, *stats)


def share_out(pieces, axis):
    return lax.all_to_all(pieces, axis, split_axis=0, concat_axis=0, tiled=True)


def swap(piece, distance):
    count = lax.axis_size("tile")
    return lax.ppermute(piece, "tile", [(i, i ^ distance) for i in range(count)])


def on_device(
    pixels,
    buckets,
    slot_owner_table,
    out_grad,
    master,
    left_stat,
    right_stat,
    left_root,
    right_root,
    vectors,
    moment,
):
    tile_count = lax.axis_size("tile")
    tile_place = lax.axis_index("tile")
    slot_count = pixels.shape[2]
    group_count = tile_count // STRIPS
    pairs = group_count // 2
    owned = master.shape[0]
    slots = owned * tile_count
    batch_count = lax.axis_size("batch")
    spot = lax.axis_index("batch").astype(jnp.int32).reshape(1)
    extra = extra_of(owned, batch_count)
    strips = share_out(pixels.reshape((tile_count,) + pixels.shape[3:]), "tile")
    dense = pack(master)
    paired = tile_count <= 8
    if paired:
        mine = [dense] + [swap(dense, 2 * k) for k in range(1, tile_count // 2)]
        pieces = mine + [swap(piece, 1) for piece in mine]
    else:
        pieces = [lax.all_gather(dense, "tile", axis=0, tiled=True)]

    numbers = jnp.arange(slots, dtype=jnp.int32)
    slot_of = jnp.sum(
        jnp.where(slot_owner_table[None, :] == numbers[:, None], numbers[None, :], 0), axis=1
    )
    owner = slot_of // owned
    within = slot_of - owner * owned
    place_of = within + (owned + extra) * owner
    if paired:
        apart = owner ^ tile_place
        apart = (apart & 1) * (tile_count // 2) + (apart >> 1)
        slot_of = within + owned * apart
        place_of = within + (owned + extra) * apart
    image_ids = lax.dynamic_index_in_dim(
        buckets.reshape(group_count, slot_count), tile_place, 1, keepdims=False
    )
    heights = jnp.where(image_ids == 0, 5 * CH // 9, jnp.where(image_ids == 1, 7 * CH // 9, CH))
    breadths = jnp.where(image_ids == 0, CW, jnp.where(image_ids == 1, 7 * CW // 9, 5 * CW // 9))
    sizes = jnp.stack([heights, breadths], axis=1).reshape(-1).astype(jnp.int32)

    two = 6 * C2 + HID2 + C2
    vec_two = jnp.concatenate([vectors[: 6 * C2], vectors[6 * C2 + HID2 : two]]).reshape(7, C2)
    vec_hid_two = vectors[6 * C2 : 6 * C2 + HID2].reshape(1, HID2)
    wide_end = two + 7 * C3
    vec_three = jnp.concatenate([vectors[two:wide_end], vectors[wide_end + HID3 :]])
    vec_three = jnp.pad(vec_three.reshape(8, C3), ((0, 0), (0, WIDE - C3)))
    vec_hid_three = vectors[wide_end : wide_end + HID3].reshape(1, HID3)

    goal = out_grad.reshape(pairs, 2, H3, W3, C3).transpose(0, 2, 3, 1, 4)
    goal = goal.reshape(pairs, H3, 2 * W3, C3)
    goal = jnp.pad(goal, ((0, 0), (0, 0), (0, LINE - 2 * W3), (0, WIDE - C3)))
    goal = goal.reshape(pairs, PLANE, WIDE)

    result, pixel_back, near, far = run_main(
        slot_of,
        place_of,
        sizes,
        strips,
        goal,
        (vec_two, vec_hid_two, vec_three, vec_hid_three),
        pieces,
        extra,
    )
    result = result[:, :, : 2 * W3, :C3].reshape(pairs, H3, W3, 2, C3).transpose(0, 3, 1, 2, 4)

    near = near.reshape(-1, owned + extra, HALF, 128)
    far = far.reshape(near.shape)
    if paired:
        own, *parts = fold_pair(near, swap(far, 1))
        pieces = [own] + [swap(part, 2 * k + 2) for k, part in enumerate(parts)]
    else:
        pieces = list(share_out(jnp.concatenate([near, far], axis=0), "tile"))
    own, *parts = fold_tile(spot, pieces, batch_count)
    pixel_back, own = lax.optimization_barrier((pixel_back, own))
    parts = [
        lax.ppermute(part, "batch", [(i, (i + k + 1) % batch_count) for i in range(batch_count)])
        for k, part in enumerate(parts)
    ]
    returned = share_out(pixel_back, "tile").astype(f32).reshape(pixels.shape)
    returned, own = lax.optimization_barrier((returned, own))
    quarter, norm = fold_batch(spot, own, parts, owned, tile_count)
    quarters = [quarter] + [
        lax.ppermute(quarter, "batch", [(i, (i + k) % batch_count) for i in range(batch_count)])
        for k in range(1, batch_count)
    ]
    norm = share_out(norm, ("batch", "tile"))
    block_grad, left_new, right_new, master_new, weight_copy, whole_vector, clip = update(
        spot, norm, quarters, extra, master, left_stat, right_stat, left_root, right_root
    )
    clip_norm = clip[0, 0]
    share = vectors.shape[0] // tile_count
    whole_vector = whole_vector.reshape(-1)
    vec_grad = lax.dynamic_slice_in_dim(whole_vector, tile_place * share, share, 0)
    vec_moment = moment + vec_grad * vec_grad
    own_vectors = lax.dynamic_slice_in_dim(vectors, tile_place * share, share, 0)
    vec_new = own_vectors - rate_vector * vec_grad / (jnp.sqrt(vec_moment) + eps_adagrad)
    return (
        result.reshape(out_grad.shape),
        returned,
        clip_norm,
        block_grad,
        left_new,
        right_new,
        master_new,
        weight_copy,
        vec_grad,
        vec_moment,
        vec_new,
    )


def solution(mesh):
    placed = (
        P("batch", "tile", None, None, None, None),
        P("batch"),
        P(),
        P("batch", "tile", None, None, None, None, None),
        P("tile", None, None),
        P("tile", None, None),
        P("tile", None, None),
        P("tile", None, None),
        P("tile", None, None),
        P(),
        P("tile"),
    )
    return jax.shard_map(
        on_device,
        mesh=mesh,
        in_specs=placed,
        out_specs=(
            P("batch", "tile", None, None, None, None, None),
            P("batch", "tile", None, None, None, None),
            P(),
            P("tile", None, None),
            P("tile", None, None),
            P("tile", None, None),
            P("tile", None, None),
            P("tile", None, None),
            P("tile"),
            P("tile"),
            P("tile"),
        ),
        check_vma=False,
    )
```

```python
import functools

import jax
import jax.numpy as jnp
from jax import lax
from jax.experimental import pallas as pl
from jax.experimental.pallas import tpu as pltpu
from jax.sharding import PartitionSpec as P

C2 = 128
HID2 = 512
C3 = 320
HID3 = 1280
CH = 36
CW = 36
STRIPS = 4
BS = 64
SR = CH // STRIPS
H3 = CH // 2
W3 = CW // 2
LONG = 7 * CH // 9
LINES = LONG // 2
WIDE = 384
LINE = 40
AREA = LINES * LINE
STEP = 2 * LINE
STEPS = AREA // STEP
HALF = BS // 2

eps_norm = 1e-05
clip_limit = 1.0
rate_matrix = 0.3
rate_vector = 0.3
eps_adagrad = 1e-08
f32 = jnp.float32
bf16 = jnp.bfloat16

SHAPES = [(C2, HID2), (HID2, C2), (9 * C2, C3), (C3, HID3), (HID3, C3)]
USED = sum(rows // BS * (cols // BS) for rows, cols in SHAPES)
VEC_ROWS = (6 * C2 + HID2 + C2 + C3 + 6 * C3 + HID3 + C3) // 128


def extra_of(owned, groups):
    extra = -(-VEC_ROWS // HALF)
    return extra + -(owned + extra) % groups


def product(left, right):
    return jnp.dot(left, right, preferred_element_type=f32)


def product_nt(left, right):
    return lax.dot_general(left, right, (((1,), (1,)), ((), ())), preferred_element_type=f32)


def product_tn(left, right):
    return lax.dot_general(left, right, (((0,), (0,)), ((), ())), preferred_element_type=f32)


def gelu_pair(values):
    bell = jnp.exp2(values * values * (-0.5 * 1.4426950408889634))
    step = pl.reciprocal(1.0 + (0.3275911 * 0.7071067811865476) * jnp.abs(values), approx=True)
    tail = step * (
        0.5 * 0.254829592
        + step
        * (
            0.5 * -0.284496736
            + step
            * (0.5 * 1.421413741 + step * (0.5 * -1.453152027 + step * (0.5 * 1.061405429)))
        )
    )
    tail = tail * bell
    share = jnp.where(values >= 0.0, 1.0 - tail, tail)
    return (values * share, share + values * (bell * 0.3989422804014327))


def fold(values):
    chans = values.shape[-1]
    return jnp.sum(values.reshape(-1, 8, chans), axis=0)


def by_image(total):
    total = total + pltpu.roll(total, 4, 0)
    total = total + pltpu.roll(total, 2, 0)
    return jnp.sum(total, axis=1, keepdims=True)


def line(pattern):
    return jnp.concatenate([pattern] * (LINE // 8), axis=0)


def spread(pattern, chans):
    return jnp.broadcast_to(pattern, (8, chans))


def affine(values, factor, shift):
    tiles = values.reshape(-1, 8, values.shape[-1])
    return (tiles * factor + shift).reshape(values.shape)


def scaled(values, factor):
    tiles = values.reshape(-1, 8, values.shape[-1])
    return (tiles * factor).reshape(values.shape)


def from_left(values):
    return pltpu.roll(values, 2, 0)


def from_right(values):
    return pltpu.roll(values, values.shape[0] - 2, 0)


def rounded(values):
    return values.astype(bf16).astype(f32)


def widen(values):
    return jnp.concatenate([values] * (WIDE // 128), axis=-1)


def norm_terms(total, square, count):
    mean = by_image(total) / count
    scaling = lax.rsqrt(by_image(square) / count - mean * mean + eps_norm)
    return (mean, scaling)


def step_rows(k, lines=0):
    return pl.ds(pl.multiple_of(k * STEP + lines * LINE, LINE), STEP)


def main_kernel(
    pairs,
    strip_count,
    slots,
    extra,
    piece_count,
    slot_ref,
    place_ref,
    size_ref,
    strips_ref,
    goal_ref,
    vec_two_ref,
    vec_hid_two_ref,
    vec_three_ref,
    vec_hid_three_ref,
    *refs,
):
    inner_kernel(
        pairs,
        strip_count,
        slots,
        extra,
        slot_ref,
        place_ref,
        size_ref,
        strips_ref,
        goal_ref,
        vec_two_ref,
        vec_hid_two_ref,
        vec_three_ref,
        vec_hid_three_ref,
        refs[:piece_count],
        *refs[piece_count:],
    )


def inner_kernel(
    pairs,
    strip_count,
    slots,
    extra,
    slot_ref,
    place_ref,
    size_ref,
    strips_ref,
    goal_ref,
    vec_two_ref,
    vec_hid_two_ref,
    vec_three_ref,
    vec_hid_three_ref,
    piece_refs,
    result_ref,
    pixel_ref,
    near_ref,
    far_ref,
    gathered_ref,
    grad_ref,
    strips,
    image_ref,
    x_ref,
    inv_ref,
    col_ref,
    pool_ref,
    mix_ref,
    zed_ref,
    dx_ref,
    hid_ref,
    u_ref,
    g_ref,
    h_ref,
    dy_ref,
    patch_ref,
    dpatch_ref,
    inv3_ref,
    e_ref,
    col3_ref,
    pool3_ref,
    mix3_ref,
    dx3_ref,
    hid3_ref,
    dhid3_ref,
    u3_ref,
    g3_ref,
    h3_ref,
    dy3_ref,
    dpre_ref,
    w1_ref,
    w2_ref,
    we_ref,
    w3_ref,
    w4_ref,
    gw1_ref,
    gw2_ref,
    gwe_ref,
    gw3_ref,
    gw4_ref,
    acc_two,
    acc_hid_two,
    acc_three,
    acc_hid_three,
    flat_ref,
    in_sem,
    out_sem,
    piece_sem,
    grad_sem,
):
    pair = pl.program_id(0)
    weights = [w1_ref, w2_ref, we_ref, w3_ref, w4_ref]
    grads = [gw1_ref, gw2_ref, gwe_ref, gw3_ref, gw4_ref]

    def strip_copies(outward):
        copies = []
        for half in range(4):
            start = lax.rem(pair * 8 + strip_count - 2 + 2 * half, strip_count)
            inside = strips.at[pl.ds(2 * half, 2)]
            if outward:
                copies.append(
                    pltpu.make_async_copy(inside, pixel_ref.at[pl.ds(start, 2)], out_sem.at[half])
                )
            else:
                copies.append(
                    pltpu.make_async_copy(strips_ref.at[pl.ds(start, 2)], inside, in_sem.at[half])
                )
        return copies

    for copy in strip_copies(False):
        copy.start()

    left_half = lax.broadcasted_iota(jnp.int32, (HALF, 128), 1) < BS

    def piece_copies():
        count = slots // len(piece_refs)
        return [
            pltpu.make_async_copy(
                ref, gathered_ref.at[pl.ds(n * count, count)], piece_sem.at[n]
            )
            for n, ref in enumerate(piece_refs)
        ]

    def grad_copies():
        half = grad_ref.shape[0] // 2
        return [
            pltpu.make_async_copy(grad_ref.at[pl.ds(n * half, half)], ref, grad_sem.at[n])
            for n, ref in enumerate((near_ref, far_ref))
        ]

    def unpack():
        for copy in piece_copies():
            copy.wait()
        offset = 0
        for (rows, cols), ref in zip(SHAPES, weights):
            wide = cols // BS
            for rb in range(rows // BS):
                for cb in range(0, wide, 2):
                    number = offset + rb * wide + cb
                    first = gathered_ref[slot_ref[number]].astype(f32)
                    turned = pltpu.roll(first, BS, 1)
                    if cb + 1 < wide:
                        second = gathered_ref[slot_ref[number + 1]].astype(f32)
                        top = jnp.where(left_half, first, pltpu.roll(second, BS, 1))
                        low = jnp.where(left_half, turned, second)
                    else:
                        top = jnp.where(left_half, first, 0.0)
                        low = jnp.where(left_half, turned, 0.0)
                    place = slice(cb * BS, cb * BS + 128)
                    ref[rb * BS : rb * BS + HALF, place] = top.astype(bf16)
                    ref[rb * BS + HALF : rb * BS + BS, place] = low.astype(bf16)
            offset += rows // BS * wide
        w3_ref[C3:, :] = jnp.zeros((WIDE - C3, HID3), bf16)

    @pl.when(pair == 0)
    def _():
        for copy in piece_copies():
            copy.start()
        unpack()
        acc_two[...] = jnp.zeros(acc_two.shape, f32)
        acc_hid_two[...] = jnp.zeros(acc_hid_two.shape, f32)
        acc_three[...] = jnp.zeros(acc_three.shape, f32)
        acc_hid_three[...] = jnp.zeros(acc_hid_three.shape, f32)

    parity = lax.broadcasted_iota(jnp.int32, (8, 128), 0) % 2
    high, broad, turned = (
        jnp.where(parity == 0, size_ref[pair * 6 + n], size_ref[pair * 6 + 3 + n])
        for n in range(3)
    )
    count_two = (high * broad * C2).astype(f32)[:, :1]
    high3 = (high + 1) // 2
    broad3 = (broad + 1) // 2
    count_three = (high3 * broad3 * C3).astype(f32)[:, :1]
    place = lax.broadcasted_iota(jnp.int32, (LINE, 128), 0) // 2
    inside = lax.broadcasted_iota(jnp.int32, (LINE, 128), 0) < 2 * W3
    reach = []
    col_share = []
    for pc in range(2):
        column = 2 * place + pc
        reach.append(jnp.where(inside & (column < line(broad)), line(high), 0))
        edge = (column == 0) | (column == line(broad) - 1)
        col_share.append(jnp.where(edge, 0.5, 1.0 / 3.0))
    reach3 = jnp.where(inside & (place < line(broad3)), line(high3), 0)
    edge3 = (place == 0) | (place == line(broad3) - 1)
    col_share3 = jnp.where(edge3, 0.5, 1.0 / 3.0)
    flipped = jnp.concatenate([turned] * (STEP // 8), axis=0) > 0

    def row_share(row, height):
        return jnp.where((row == 0) | (row == height - 1), 0.5, 1.0 / 3.0)

    def inverse_count(row, reach, col_share, height):
        return jnp.where(row < reach, line(row_share(row, height)) * col_share, 0.0)

    gain1, bias1, scale1 = (vec_two_ref[n : n + 1] for n in range(3))
    gain2, bias2, scale2, out_bias = (vec_two_ref[n : n + 1] for n in range(3, 7))
    embed_bias, gain3, bias3, scale3 = (vec_three_ref[n : n + 1] for n in range(4))
    gain4, bias4, scale4, out_bias3 = (vec_three_ref[n : n + 1] for n in range(4, 8))

    for copy in strip_copies(False):
        copy.wait()

    zero_line = jnp.zeros((LINE, C2), f32)
    zero_line3 = jnp.zeros((LINE, WIDE), f32)
    for plane in range(4):
        col_ref[plane, 0:LINE] = zero_line
        col_ref[plane, AREA + LINE : AREA + 2 * LINE] = zero_line
        zed_ref[plane, 0:LINE] = zero_line
    col3_ref[0:LINE] = zero_line3
    col3_ref[AREA + LINE : AREA + 2 * LINE] = zero_line3

    def to_rows(within, carry):
        for spot in range(2 * STRIPS):
            image, strip = spot // STRIPS, spot % STRIPS
            start = pl.multiple_of((strip * SR + within) * LINE, LINE)
            image_ref[image, pl.ds(start, CW)] = strips[spot, within].astype(f32)
        return carry

    lax.fori_loop(0, SR, to_rows, 0)

    def plane_places(image, flat, r):
        for pr in range(2):
            for pc in range(2):
                line_place = pl.ds(r * LINE + image, W3, stride=2)
                if flat:
                    there = pl.ds((2 * r + pr) * LINE + pc, W3, stride=2)
                else:
                    there = pl.ds(pc * LINE + 2 * r + pr, W3, stride=2 * LINE)
                yield (pr * 2 + pc, line_place, there)

    def each_image(visit):
        for image in range(2):
            way = size_ref[pair * 6 + 3 * image + 2]
            for flat in (True, False):

                @pl.when(way == (0 if flat else 1))
                def _():
                    def one(r, carry):
                        for plane, line_place, there in plane_places(image, flat, r):
                            visit(image, plane, line_place, there)
                        return carry

                    lax.fori_loop(0, LINES, one, 0)

    def take_in(image, plane, line_place, there):
        x_ref[plane, line_place] = image_ref[image, there]

    each_image(take_in)

    def arrange(k, carry):
        total, square = carry
        rows = step_rows(k)
        for plane in range(4):
            pr, pc = plane // 2, plane % 2
            share = jnp.concatenate(
                [
                    inverse_count(4 * k + 2 * n + pr, reach[pc], col_share[pc], high)
                    for n in range(2)
                ],
                axis=0,
            )
            inv_ref[plane, rows] = share
            values = jnp.where(share > 0.0, x_ref[plane, rows], 0.0)
            x_ref[plane, rows] = values
            total = total + fold(values)
            square = square + fold(values * values)
        inv3_ref[rows] = jnp.concatenate(
            [inverse_count(2 * k + n, reach3, col_share3, high3) for n in range(2)], axis=0
        )
        return (total, square)

    nothing = jnp.zeros((8, C2), f32)
    nothing3 = jnp.zeros((8, WIDE), f32)
    total, square = lax.fori_loop(0, STEPS, arrange, (nothing, nothing))
    mean1, scaling1 = norm_terms(total, square, count_two)
    factor1 = scaling1 * gain1
    shift1 = bias1 - mean1 * scaling1 * gain1

    def window_cols(k, carry):
        rows = step_rows(k)
        for pr in range(2):
            masked = []
            for pc in range(2):
                plane = pr * 2 + pc
                normal = rounded(affine(x_ref[plane, rows], factor1, shift1))
                masked.append(jnp.where(inv_ref[plane, rows] > 0.0, normal, 0.0))
            both = masked[0] + masked[1]
            col_ref[pr * 2, step_rows(k, 1)] = both + from_left(masked[1])
            col_ref[pr * 2 + 1, step_rows(k, 1)] = both + from_right(masked[0])
        return carry

    lax.fori_loop(0, STEPS, window_cols, 0)

    def row_windows(pc, k):
        both = col_ref[pc, step_rows(k, 1)] + col_ref[2 + pc, step_rows(k, 1)]
        return (both + col_ref[2 + pc, step_rows(k)], both + col_ref[pc, step_rows(k, 2)])

    def mix(k, carry):
        total, square = carry
        rows = step_rows(k)
        for pc in range(2):
            windows = row_windows(pc, k)
            for pr in range(2):
                plane = pr * 2 + pc
                values = x_ref[plane, rows]
                share = inv_ref[plane, rows]
                pooled = windows[pr] * share - rounded(affine(values, factor1, shift1))
                pooled = jnp.where(share > 0.0, pooled, 0.0)
                mixed = values + scale1 * pooled
                pool_ref[plane, rows] = pooled
                mix_ref[plane, rows] = mixed
                total = total + fold(mixed)
                square = square + fold(mixed * mixed)
        return (total, square)

    total, square = lax.fori_loop(0, STEPS, mix, (nothing, nothing))
    mean2, scaling2 = norm_terms(total, square, count_two)
    factor2 = scaling2 * gain2
    shift2 = bias2 - mean2 * scaling2 * gain2

    def plane_rows(plane):
        return pl.ds(pl.multiple_of(plane * AREA, AREA), AREA)

    def branch(plane, carry):
        mixed = mix_ref[plane]
        low = affine(mixed, factor2, shift2).astype(bf16)
        h_ref[plane_rows(plane)] = low
        hid_ref[...] = product(low, w1_ref[...])

        def activate(k, carry):
            rows = step_rows(k)
            flat = pl.ds(pl.multiple_of(plane * AREA + k * STEP, STEP), STEP)
            for at in range(0, HID2, 128):
                lanes = slice(at, at + 128)
                active, slope = gelu_pair(hid_ref[rows, lanes] + vec_hid_two_ref[:, lanes])
                u_ref[flat, lanes] = active.astype(bf16)
                g_ref[flat, lanes] = slope.astype(bf16)
            return carry

        lax.fori_loop(0, STEPS, activate, 0)
        out = product(u_ref[plane_rows(plane)], w2_ref[...]) + out_bias
        zed = jnp.where(inv_ref[plane] > 0.0, mixed + scale2 * out, 0.0)
        zed_ref[plane, LINE : LINE + AREA] = rounded(zed)
        return carry

    lax.fori_loop(0, 4, branch, 0)

    def patches(k, carry):
        rows = step_rows(k)
        taps = []
        for ky in range(3):
            pr = (0 if ky == 1 else 1) * 2
            source = step_rows(k, 0 if ky == 0 else 1)
            even = zed_ref[pr, source]
            odd = zed_ref[pr + 1, source]
            taps.append((from_left(odd), even, odd))
        for ky in range(3):
            for kx in range(3):
                at = (3 * ky + kx) * C2
                tap = taps[ky][kx]
                if ky != kx:
                    tap = jnp.where(flipped, taps[kx][ky], tap)
                patch_ref[rows, at : at + C2] = tap.astype(bf16)
        return carry

    lax.fori_loop(0, STEPS, patches, 0)
    e_ref[...] = product(patch_ref[...], we_ref[...])

    def embed(k, carry):
        total, square = carry
        rows = step_rows(k)
        out = jnp.where(widen(inv3_ref[rows]) > 0.0, e_ref[rows] + embed_bias, 0.0)
        e_ref[rows] = out
        return (total + fold(out), square + fold(out * out))

    total, square = lax.fori_loop(0, STEPS, embed, (nothing3, nothing3))
    mean3, scaling3 = norm_terms(total, square, count_three)
    factor3 = scaling3 * gain3
    shift3 = bias3 - mean3 * scaling3 * gain3

    def window_cols3(k, carry):
        rows = step_rows(k)
        normal = rounded(affine(e_ref[rows], factor3, shift3))
        masked = jnp.where(widen(inv3_ref[rows]) > 0.0, normal, 0.0)
        col3_ref[step_rows(k, 1)] = masked + from_left(masked) + from_right(masked)
        return carry

    lax.fori_loop(0, STEPS, window_cols3, 0)

    def row_windows3(k):
        return col3_ref[step_rows(k)] + col3_ref[step_rows(k, 1)] + col3_ref[step_rows(k, 2)]

    def mix3(k, carry):
        total, square = carry
        rows = step_rows(k)
        values = e_ref[rows]
        share = widen(inv3_ref[rows])
        pooled = row_windows3(k) * share - rounded(affine(values, factor3, shift3))
        pooled = jnp.where(share > 0.0, pooled, 0.0)
        mixed = values + scale3 * pooled
        pool3_ref[rows] = pooled
        mix3_ref[rows] = mixed
        return (total + fold(mixed), square + fold(mixed * mixed))

    total, square = lax.fori_loop(0, STEPS, mix3, (nothing3, nothing3))
    mean4, scaling4 = norm_terms(total, square, count_three)
    factor4 = scaling4 * gain4
    shift4 = bias4 - mean4 * scaling4 * gain4
    normal4 = (spread(scaling4, WIDE), spread(-mean4 * scaling4, WIDE))

    def prepare3(k, d_bias):
        rows = step_rows(k)
        h3_ref[rows] = affine(mix3_ref[rows], factor4, shift4).astype(bf16)
        goal = goal_ref[0, rows].astype(f32)
        goal = jnp.where(widen(inv3_ref[rows]) > 0.0, goal, 0.0)
        low_goal = (scale4 * goal).astype(bf16)
        dy3_ref[rows] = low_goal
        return d_bias + fold(low_goal.astype(f32))

    acc_three[7] += lax.fori_loop(0, STEPS, prepare3, nothing3)
    hid3_ref[...] = product(h3_ref[...], w3_ref[...])
    dhid3_ref[...] = product_nt(dy3_ref[...], w4_ref[...])

    def activate3(k, sums):
        rows = step_rows(k)
        new = []
        for n, at in enumerate(range(0, HID3, 128)):
            lanes = slice(at, at + 128)
            active, slope = gelu_pair(hid3_ref[rows, lanes] + vec_hid_three_ref[:, lanes])
            u3_ref[rows, lanes] = active.astype(bf16)
            low = (slope * dhid3_ref[rows, lanes]).astype(bf16)
            g3_ref[rows, lanes] = low
            new.append(sums[n] + fold(low.astype(f32)))
        return tuple(new)

    sums = lax.fori_loop(0, STEPS, activate3, (nothing,) * (HID3 // 128))
    for n, value in enumerate(sums):
        acc_hid_three[:, n * 128 : n * 128 + 128] += value

    def keep(ref, value):
        if pairs == 1:
            ref[...] = value
        else:

            @pl.when(pair == 0)
            def _():
                ref[...] = value

            @pl.when(pair > 0)
            def _():
                ref[...] += value

    result_ref[0] = product(u3_ref[...], w4_ref[...])
    dx3_ref[...] = product_nt(g3_ref[...], w3_ref[...])
    keep(gw3_ref, product_tn(h3_ref[...], g3_ref[...]))
    keep(gw4_ref, product_tn(u3_ref[...], dy3_ref[...]))

    def finish3(k, carry):
        d_scale, d_shift, d_gain = carry
        rows = step_rows(k)
        valid = widen(inv3_ref[rows]) > 0.0
        mixed = mix3_ref[rows]
        out = jnp.where(valid, result_ref[0, rows] + out_bias3, 0.0)
        result_ref[0, rows] = mixed + scale4 * out
        d_scale = d_scale + fold(out * goal_ref[0, rows].astype(f32))
        d_low = dx3_ref[rows]
        normal = affine(mixed, *normal4)
        return (d_scale, d_shift + fold(d_low), d_gain + fold(d_low * normal))

    d_scale, d_shift, d_gain = lax.fori_loop(0, STEPS, finish3, (nothing3, nothing3, nothing3))
    acc_three[6] += d_scale
    acc_three[5] += d_shift
    acc_three[4] += d_gain
    mean_shift = by_image(d_shift * gain4) / count_three
    mean_gain = by_image(d_gain * gain4) / count_three
    back_gain4 = scaling4 * gain4
    back_mean4 = spread(-scaling4 * mean_shift, WIDE)
    back_normal4 = spread(scaling4 * mean_gain, WIDE)

    def unmix3(k, d_scale):
        rows = step_rows(k)
        share = widen(inv3_ref[rows])
        valid = share > 0.0
        normal = affine(mix3_ref[rows], *normal4)
        back = affine(dx3_ref[rows], back_gain4, back_mean4) - scaled(normal, back_normal4)
        d_mixed = jnp.where(valid, back + goal_ref[0, rows].astype(f32), 0.0)
        dx3_ref[rows] = d_mixed
        d_scale = d_scale + fold(pool3_ref[rows] * d_mixed)
        weighted = scale3 * d_mixed * share
        col3_ref[step_rows(k, 1)] = weighted + from_left(weighted) + from_right(weighted)
        return d_scale

    acc_three[3] += lax.fori_loop(0, STEPS, unmix3, nothing3)
    normal3 = (spread(scaling3, WIDE), spread(-mean3 * scaling3, WIDE))

    def unpool3(k, carry):
        d_shift, d_gain = carry
        rows = step_rows(k)
        valid = widen(inv3_ref[rows]) > 0.0
        d_normal = jnp.where(valid, row_windows3(k) - scale3 * dx3_ref[rows], 0.0)
        pool3_ref[rows] = d_normal
        normal = affine(e_ref[rows], *normal3)
        return (d_shift + fold(d_normal), d_gain + fold(d_normal * normal))

    d_shift, d_gain = lax.fori_loop(0, STEPS, unpool3, (nothing3, nothing3))
    acc_three[2] += d_shift
    acc_three[1] += d_gain
    mean_shift = by_image(d_shift * gain3) / count_three
    mean_gain = by_image(d_gain * gain3) / count_three
    back_gain3 = scaling3 * gain3
    back_mean3 = spread(-scaling3 * mean_shift, WIDE)
    back_normal3 = spread(scaling3 * mean_gain, WIDE)

    def unnorm3(k, d_bias):
        rows = step_rows(k)
        valid = widen(inv3_ref[rows]) > 0.0
        normal = affine(e_ref[rows], *normal3)
        back = affine(pool3_ref[rows], back_gain3, back_mean3) - scaled(normal, back_normal3)
        low = jnp.where(valid, dx3_ref[rows] + back, 0.0).astype(bf16)
        dpre_ref[rows] = low
        return d_bias + fold(low.astype(f32))

    acc_three[0] += lax.fori_loop(0, STEPS, unnorm3, nothing3)
    keep(gwe_ref, product_tn(patch_ref[...], dpre_ref[...]))
    dpatch_ref[0:AREA] = product_nt(dpre_ref[...], we_ref[...])
    dpatch_ref[AREA : AREA + LINE] = jnp.zeros((LINE, 9 * C2), f32)

    def gather_back(k, carry):
        rows = step_rows(k)

        def tap(ky, kx, source):
            at = (3 * ky + kx) * C2
            value = dpatch_ref[source, at : at + C2]
            if ky != kx:
                at = (3 * kx + ky) * C2
                value = jnp.where(flipped, dpatch_ref[source, at : at + C2], value)
            return value

        sources = []
        for ky in range(3):
            source = step_rows(k, 1 if ky == 0 else 0)
            sources.append(
                (tap(ky, 1, source), tap(ky, 2, source) + from_right(tap(ky, 0, source)))
            )
        for pc in range(2):
            for pr, value in ((0, sources[1][pc]), (1, sources[2][pc] + sources[0][pc])):
                plane = pr * 2 + pc
                valid = inv_ref[plane, rows] > 0.0
                zed_ref[plane, rows] = jnp.where(valid, rounded(value), 0.0)
        return carry

    lax.fori_loop(0, STEPS, gather_back, 0)

    normal2 = (spread(scaling2, C2), spread(-mean2 * scaling2, C2))

    def unbranch(plane, carry):
        d_out_bias, d_shift, d_gain, sums = carry
        flat = plane_rows(plane)
        low_goal = (scale2 * zed_ref[plane, 0:AREA]).astype(bf16)
        dy_ref[flat] = low_goal
        hid_ref[...] = product_nt(low_goal, w2_ref[...])

        def slopes(k, sums):
            rows = step_rows(k)
            part = pl.ds(pl.multiple_of(plane * AREA + k * STEP, STEP), STEP)
            new = []
            for n, at in enumerate(range(0, HID2, 128)):
                lanes = slice(at, at + 128)
                low = (g_ref[part, lanes].astype(f32) * hid_ref[rows, lanes]).astype(bf16)
                g_ref[part, lanes] = low
                new.append(sums[n] + fold(low.astype(f32)))
            return tuple(new)

        sums = lax.fori_loop(0, STEPS, slopes, sums)
        d_low = product_nt(g_ref[flat], w1_ref[...])
        dx_ref[plane] = d_low
        normal = affine(mix_ref[plane], *normal2)
        return (
            d_out_bias + fold(low_goal.astype(f32)),
            d_shift + fold(d_low),
            d_gain + fold(d_low * normal),
            sums,
        )

    d_out_bias, d_shift, d_gain, sums = lax.fori_loop(
        0, 4, unbranch, (nothing, nothing, nothing, (nothing,) * (HID2 // 128))
    )
    for n, value in enumerate(sums):
        acc_hid_two[:, n * 128 : n * 128 + 128] += value
    acc_two[6] += d_out_bias
    acc_two[4] += d_shift
    acc_two[3] += d_gain
    mean_shift = by_image(d_shift * gain2) / count_two
    mean_gain = by_image(d_gain * gain2) / count_two
    keep(gw1_ref, product_tn(h_ref[...], g_ref[...]))
    new_gw2 = product_tn(dy_ref[...], u_ref[...]).T
    keep(gw2_ref, new_gw2)
    d_scale = fold(w2_ref[...].astype(f32) * new_gw2) + out_bias * d_out_bias
    acc_two[5] += d_scale / scale2

    back_gain2 = scaling2 * gain2
    back_mean2 = spread(-scaling2 * mean_shift, C2)
    back_normal2 = spread(scaling2 * mean_gain, C2)

    def unmix(k, d_scale):
        rows = step_rows(k)
        for pr in range(2):
            weighted = []
            for pc in range(2):
                plane = pr * 2 + pc
                share = inv_ref[plane, rows]
                normal = affine(mix_ref[plane, rows], *normal2)
                back = affine(dx_ref[plane, rows], back_gain2, back_mean2)
                back = back - scaled(normal, back_normal2)
                d_mixed = jnp.where(share > 0.0, zed_ref[plane, rows] + back, 0.0)
                dx_ref[plane, rows] = d_mixed
                d_scale = d_scale + fold(pool_ref[plane, rows] * d_mixed)
                weighted.append(scale1 * d_mixed * share)
            both = weighted[0] + weighted[1]
            col_ref[pr * 2, step_rows(k, 1)] = both + from_left(weighted[1])
            col_ref[pr * 2 + 1, step_rows(k, 1)] = both + from_right(weighted[0])
        return d_scale

    acc_two[2] += lax.fori_loop(0, STEPS, unmix, nothing)
    normal1 = (spread(scaling1, C2), spread(-mean1 * scaling1, C2))

    def unpool(k, carry):
        d_shift, d_gain = carry
        rows = step_rows(k)
        for pc in range(2):
            windows = row_windows(pc, k)
            for pr in range(2):
                plane = pr * 2 + pc
                valid = inv_ref[plane, rows] > 0.0
                d_normal = windows[pr] - scale1 * dx_ref[plane, rows]
                d_normal = jnp.where(valid, d_normal, 0.0)
                pool_ref[plane, rows] = d_normal
                normal = affine(x_ref[plane, rows], *normal1)
                d_shift = d_shift + fold(d_normal)
                d_gain = d_gain + fold(d_normal * normal)
        return (d_shift, d_gain)

    d_shift, d_gain = lax.fori_loop(0, STEPS, unpool, (nothing, nothing))
    acc_two[1] += d_shift
    acc_two[0] += d_gain
    mean_shift = by_image(d_shift * gain1) / count_two
    mean_gain = by_image(d_gain * gain1) / count_two
    back_gain1 = scaling1 * gain1
    back_mean1 = spread(-scaling1 * mean_shift, C2)
    back_normal1 = spread(scaling1 * mean_gain, C2)

    def unnorm(k, carry):
        rows = step_rows(k)
        for plane in range(4):
            normal = affine(x_ref[plane, rows], *normal1)
            back = affine(pool_ref[plane, rows], back_gain1, back_mean1)
            back = back - scaled(normal, back_normal1)
            valid = inv_ref[plane, rows] > 0.0
            dx_ref[plane, rows] = jnp.where(valid, dx_ref[plane, rows] + back, 0.0)
        return carry

    lax.fori_loop(0, STEPS, unnorm, 0)

    def give_back(image, plane, line_place, there):
        image_ref[image, there] = dx_ref[plane, line_place]

    image_ref[...] = jnp.zeros(image_ref.shape, f32)
    each_image(give_back)

    def from_rows(within, carry):
        for spot in range(2 * STRIPS):
            image, strip = spot // STRIPS, spot % STRIPS
            start = pl.multiple_of((strip * SR + within) * LINE, LINE)
            strips[spot, within] = image_ref[image, pl.ds(start, CW)].astype(bf16)
        return carry

    lax.fori_loop(0, SR, from_rows, 0)
    for copy in strip_copies(True):
        copy.start()

    @pl.when(pair == pairs - 1)
    def _():
        offset = 0
        for (rows, cols), ref in zip(SHAPES, grads):
            wide = cols // BS
            for rb in range(rows // BS):
                for cb in range(0, wide, 2):
                    number = offset + rb * wide + cb
                    at = slice(cb * BS, cb * BS + 128)
                    top = ref[rb * BS : rb * BS + HALF, at]
                    low = ref[rb * BS + HALF : rb * BS + BS, at]
                    grad_ref[place_ref[number]] = jnp.where(
                        left_half, top, pltpu.roll(low, BS, 1)
                    ).astype(bf16)
                    if cb + 1 < wide:
                        grad_ref[place_ref[number + 1]] = jnp.where(
                            left_half, pltpu.roll(top, BS, 1), low
                        ).astype(bf16)
            offset += rows // BS * wide

        def filler(number, carry):
            grad_ref[place_ref[number]] = jnp.zeros((HALF, 128), bf16)
            return carry

        lax.fori_loop(USED, slots, filler, 0)

        flat_ref[...] = jnp.zeros(flat_ref.shape, f32)

        def put(at, total, length):
            if at % 128:
                room = jnp.zeros((8, 128), f32)
                if total.shape[1] < length + BS:
                    total = jnp.concatenate([total, room], axis=1)
                total = pltpu.roll(total, BS, 1)
            whole = jnp.sum(total, axis=0, keepdims=True)
            done = -(at % 128)
            row = at // 128
            lane = 0
            while done < length:
                first = max(0, -done)
                last = min(128, length - done)
                flat_ref[row : row + 1, first:last] = whole[:, lane + first : lane + last]
                done += 128
                lane += 128
                row += 1

        at = 0
        for n in range(6):
            put(at, acc_two[n], C2)
            at += C2
        put(at, acc_hid_two[...], HID2)
        at += HID2
        put(at, acc_two[6], C2)
        at += C2
        for n in range(7):
            put(at, acc_three[n], C3)
            at += C3
        put(at, acc_hid_three[...], HID3)
        at += HID3
        put(at, acc_three[7], C3)
        packed = flat_ref[...].astype(bf16)
        stride = slots // strip_count + extra
        for n in range(extra):
            piece = packed[n * HALF : (n + 1) * HALF]

            def leave(target, carry):
                grad_ref[target * stride + stride - extra + n] = piece
                return carry

            lax.fori_loop(0, strip_count, leave, 0)
        for copy in grad_copies():
            copy.start()
        for copy in grad_copies():
            copy.wait()

    for copy in strip_copies(True):
        copy.wait()


def run_main(slot_of, place_of, sizes, strips, goal, vectors, pieces, extra):
    strip_count = strips.shape[0]
    pairs = goal.shape[0]
    slots = sum(piece.shape[0] for piece in pieces)
    rows_out = slots + extra * strip_count

    def whole(shape):
        return pl.BlockSpec(shape, lambda t: (0,) * len(shape), pipeline_mode=pl.Buffered(1))

    smem = pl.BlockSpec(memory_space=pltpu.SMEM)
    anywhere = pl.BlockSpec(memory_space=pl.ANY)
    plane_f32 = pltpu.VMEM((4, AREA, C2), f32)
    wide_f32 = pltpu.VMEM((AREA, WIDE), f32)
    wide_bf16 = pltpu.VMEM((AREA, WIDE), bf16)
    scratch = [
        pltpu.VMEM((slots, HALF, 128), bf16),
        pltpu.VMEM((rows_out, HALF, 128), bf16),
        pltpu.VMEM((2 * STRIPS, SR, CW, C2), bf16),
        pltpu.VMEM((2, CH * LINE, C2), f32),
        plane_f32,
        plane_f32,
        pltpu.VMEM((4, AREA + 2 * LINE, C2), f32),
        plane_f32,
        plane_f32,
        pltpu.VMEM((4, AREA + LINE, C2), f32),
        plane_f32,
        pltpu.VMEM((AREA, HID2), f32),
        pltpu.VMEM((4 * AREA, HID2), bf16),
        pltpu.VMEM((4 * AREA, HID2), bf16),
        pltpu.VMEM((4 * AREA, C2), bf16),
        pltpu.VMEM((4 * AREA, C2), bf16),
        pltpu.VMEM((AREA, 9 * C2), bf16),
        pltpu.VMEM((AREA + LINE, 9 * C2), f32),
        pltpu.VMEM((AREA, 128), f32),
        wide_f32,
        pltpu.VMEM((AREA + 2 * LINE, WIDE), f32),
        wide_f32,
        wide_f32,
        wide_f32,
        pltpu.VMEM((AREA, HID3), f32),
        pltpu.VMEM((AREA, HID3), f32),
        pltpu.VMEM((AREA, HID3), bf16),
        pltpu.VMEM((AREA, HID3), bf16),
        wide_bf16,
        wide_bf16,
        wide_bf16,
        pltpu.VMEM((C2, HID2), bf16),
        pltpu.VMEM((HID2, C2), bf16),
        pltpu.VMEM((9 * C2, WIDE), bf16),
        pltpu.VMEM((WIDE, HID3), bf16),
        pltpu.VMEM((HID3, WIDE), bf16),
        pltpu.VMEM((C2, HID2), f32),
        pltpu.VMEM((HID2, C2), f32),
        pltpu.VMEM((9 * C2, WIDE), f32),
        pltpu.VMEM((WIDE, HID3), f32),
        pltpu.VMEM((HID3, WIDE), f32),
        pltpu.VMEM((7, 8, C2), f32),
        pltpu.VMEM((8, HID2), f32),
        pltpu.VMEM((8, 8, WIDE), f32),
        pltpu.VMEM((8, HID3), f32),
        pltpu.VMEM((extra * HALF, 128), f32),
        pltpu.SemaphoreType.DMA((4,)),
        pltpu.SemaphoreType.DMA((4,)),
        pltpu.SemaphoreType.DMA((len(pieces),)),
        pltpu.SemaphoreType.DMA((2,)),
    ]
    return pl.pallas_call(
        functools.partial(main_kernel, pairs, strip_count, slots, extra, len(pieces)),
        grid=(pairs,),
        in_specs=[
            smem,
            smem,
            smem,
            anywhere,
            pl.BlockSpec((1,) + goal.shape[1:], lambda t: (t, 0, 0)),
        ]
        + [whole(vector.shape) for vector in vectors]
        + [anywhere] * len(pieces),
        out_specs=[
            pl.BlockSpec((1, AREA, WIDE), lambda t: (t, 0, 0)),
            anywhere,
            anywhere,
            anywhere,
        ],
        out_shape=[
            jax.ShapeDtypeStruct((pairs, AREA, WIDE), f32),
            jax.ShapeDtypeStruct(strips.shape, bf16),
            jax.ShapeDtypeStruct((rows_out // 2, HALF, 128), bf16),
            jax.ShapeDtypeStruct((rows_out // 2, HALF, 128), bf16),
        ],
        scratch_shapes=scratch,
        compiler_params=pltpu.CompilerParams(vmem_limit_bytes=62 * 1024 * 1024),
        name="blocks",
    )(slot_of, place_of, sizes, strips, goal, *vectors, *pieces)


def pack_kernel(master_ref, dense_ref):
    values = master_ref[...]
    dense_ref[...] = jnp.concatenate([values[:, :HALF], values[:, HALF:]], axis=2).astype(bf16)


def pack(master):
    owned = master.shape[0]
    return pl.pallas_call(
        pack_kernel,
        out_shape=jax.ShapeDtypeStruct((owned, HALF, 2 * BS), bf16),
        name="pack",
    )(master)


def fold_pair_kernel(near_ref, got_ref, own_ref, *part_refs):
    for n in range(len(part_refs) + 1):
        total = near_ref[n].astype(f32) + got_ref[n].astype(f32)
        if n == 0:
            own_ref[...] = total
        else:
            part_refs[n - 1][...] = total.astype(bf16)


def fold_pair(near, got):
    part = jax.ShapeDtypeStruct(near.shape[1:], bf16)
    own = jax.ShapeDtypeStruct(near.shape[1:], f32)
    return pl.pallas_call(
        fold_pair_kernel,
        out_shape=[own] + [part] * (near.shape[0] - 1),
        name="fold_pair",
    )(near, got)


def fold_tile_kernel(pieces, spot_ref, *refs):
    piece_refs, (own_ref, *part_refs) = refs[:pieces], refs[pieces:]
    groups = len(part_refs) + 1
    share = own_ref.shape[0]
    for k in range(groups):
        start = lax.rem(spot_ref[0] + k, groups) * share
        total = piece_refs[0][pl.ds(start, share)].astype(f32)
        for ref in piece_refs[1:]:
            total = total + ref[pl.ds(start, share)].astype(f32)
        if k == 0:
            own_ref[...] = total
        else:
            part_refs[k - 1][...] = total.astype(bf16)


def fold_tile(spot, pieces, groups):
    share = pieces[0].shape[0] // groups
    part = jax.ShapeDtypeStruct((share,) + pieces[0].shape[1:], bf16)
    own = jax.ShapeDtypeStruct(part.shape, f32)
    return pl.pallas_call(
        functools.partial(fold_tile_kernel, len(pieces)),
        in_specs=[pl.BlockSpec(memory_space=pltpu.SMEM)]
        + [pl.BlockSpec(memory_space=pltpu.VMEM)] * len(pieces),
        out_shape=[own] + [part] * (groups - 1),
        name="fold_tile",
    )(spot, *pieces)


def fold_batch_kernel(owned, vector_weight, spot_ref, own_ref, *refs):
    part_refs, (total_ref, norm_ref) = refs[:-2], refs[-2:]
    share = own_ref.shape[0]
    square = jnp.zeros((8, 128), f32)
    for n in range(share):
        total = own_ref[n]
        for ref in part_refs:
            total = total + ref[n].astype(f32)
        total_ref[n] = total.astype(bf16)
        weight = jnp.where(spot_ref[0] * share + n < owned, 1.0, vector_weight)
        square = square + weight * fold(total * total)
    square = jnp.sum(jnp.sum(square, axis=1, keepdims=True), axis=0, keepdims=True)
    norm_ref[...] = jnp.broadcast_to(square[None], norm_ref.shape)


def fold_batch(spot, own, parts, owned, tile_count):
    count = tile_count * (len(parts) + 1)
    vmem = pl.BlockSpec(memory_space=pltpu.VMEM)
    return pl.pallas_call(
        functools.partial(fold_batch_kernel, owned, 1.0 / tile_count),
        in_specs=[pl.BlockSpec(memory_space=pltpu.SMEM)] + [vmem] * (len(parts) + 1),
        out_shape=[
            jax.ShapeDtypeStruct(own.shape, bf16),
            jax.ShapeDtypeStruct((count, 1, 128), f32),
        ],
        name="fold_batch",
    )(spot, own, *parts)


def update_kernel(owned, groups, spot_ref, norm_ref, *refs):
    quarters = refs[:groups]
    (
        master_ref,
        left_stat_ref,
        right_stat_ref,
        left_root_ref,
        right_root_ref,
        grad_ref,
        left_ref,
        right_ref,
        new_ref,
        copy_ref,
        vector_ref,
        clip_ref,
    ) = refs[groups:]
    share = quarters[0].shape[0]
    part = grad_ref.shape[0]
    step = pl.program_id(0)
    norm = jnp.sqrt(jnp.sum(norm_ref[...], axis=0))
    factor = jnp.minimum(1.0, clip_limit / norm)

    def summed(number):
        source = number // share
        local = number - source * share
        turn = lax.rem(spot_ref[0] - source + groups, groups)
        value = quarters[0][local].astype(f32)
        for k in range(1, groups):
            value = jnp.where(turn == k, quarters[k][local].astype(f32), value)
        return value * factor

    @pl.when(step == 0)
    def _():
        clip_ref[...] = norm
        for n in range(vector_ref.shape[0]):
            vector_ref[n] = summed(owned + n)

    for n in range(part):
        dense = summed(jnp.minimum(step * part + n, owned - 1))
        grad = jnp.concatenate([dense[:, :BS], dense[:, BS:]], axis=0)
        grad_ref[n] = grad
        low = grad.astype(bf16)
        left_ref[n] = 0.5 * left_stat_ref[n] + 0.5 * product_nt(low, low)
        right_ref[n] = 0.5 * right_stat_ref[n] + 0.5 * product_tn(low, low)
        stepped = product(left_root_ref[n].astype(bf16), low).astype(bf16)
        stepped = product(stepped, right_root_ref[n].astype(bf16))
        new = master_ref[n] - rate_matrix * stepped
        new_ref[n] = new
        copy_ref[n] = new.astype(bf16)


def update(spot, norm, quarters, extra, master, *stats):
    owned = master.shape[0]
    part = min(owned, 7)
    groups = len(quarters)
    square = pl.BlockSpec((part, BS, BS), lambda t: (t, 0, 0))
    shape = jax.ShapeDtypeStruct(master.shape, f32)

    def whole(shape):
        return pl.BlockSpec(shape, lambda t: (0,) * len(shape))

    return pl.pallas_call(
        functools.partial(update_kernel, owned, groups),
        grid=(-(-owned // part),),
        in_specs=[pl.BlockSpec(memory_space=pltpu.SMEM), whole(norm.shape)]
        + [whole(quarters[0].shape)] * groups
        + [square] * 5,
        out_specs=[square] * 5 + [whole((extra, HALF, 128)), whole((1, 128))],
        out_shape=[shape] * 4
        + [
            jax.ShapeDtypeStruct(master.shape, bf16),
            jax.ShapeDtypeStruct((extra, HALF, 128), f32),
            jax.ShapeDtypeStruct((1, 128), f32),
        ],
        compiler_params=pltpu.CompilerParams(vmem_limit_bytes=32 * 1024 * 1024),
        name="update",
    )(spot, norm, *quarters, master, *stats)


def share_out(pieces, axis):
    return lax.all_to_all(pieces, axis, split_axis=0, concat_axis=0, tiled=True)


def swap(piece, distance):
    count = lax.axis_size("tile")
    return lax.ppermute(piece, "tile", [(i, i ^ distance) for i in range(count)])


def on_device(
    pixels,
    buckets,
    slot_owner_table,
    out_grad,
    master,
    left_stat,
    right_stat,
    left_root,
    right_root,
    vectors,
    moment,
):
    tile_count = lax.axis_size("tile")
    tile_place = lax.axis_index("tile")
    slot_count = pixels.shape[2]
    group_count = tile_count // STRIPS
    pairs = group_count // 2
    owned = master.shape[0]
    slots = owned * tile_count
    batch_count = lax.axis_size("batch")
    spot = lax.axis_index("batch").astype(jnp.int32).reshape(1)
    extra = extra_of(owned, batch_count)
    strips = share_out(pixels.reshape((tile_count,) + pixels.shape[3:]), "tile")
    dense = pack(master)
    paired = tile_count <= 8
    if paired:
        mine = [dense] + [swap(dense, 2 * k) for k in range(1, tile_count // 2)]
        pieces = mine + [swap(piece, 1) for piece in mine]
    else:
        pieces = [lax.all_gather(dense, "tile", axis=0, tiled=True)]

    numbers = jnp.arange(slots, dtype=jnp.int32)
    slot_of = jnp.sum(
        jnp.where(slot_owner_table[None, :] == numbers[:, None], numbers[None, :], 0), axis=1
    )
    owner = slot_of // owned
    within = slot_of - owner * owned
    place_of = within + (owned + extra) * owner
    if paired:
        apart = owner ^ tile_place
        apart = (apart & 1) * (tile_count // 2) + (apart >> 1)
        slot_of = within + owned * apart
        place_of = within + (owned + extra) * apart
    image_ids = lax.dynamic_index_in_dim(
        buckets.reshape(group_count, slot_count), tile_place, 1, keepdims=False
    )
    turned = image_ids >= 2
    heights = jnp.where(image_ids == 0, 5 * CH // 9, jnp.where(image_ids == 1, 7 * CH // 9, CH))
    breadths = jnp.where(image_ids == 0, CW, jnp.where(image_ids == 1, 7 * CW // 9, 5 * CW // 9))
    sizes = jnp.stack(
        [
            jnp.where(turned, breadths, heights),
            jnp.where(turned, heights, breadths),
            turned,
        ],
        axis=1,
    )
    sizes = sizes.reshape(-1).astype(jnp.int32)

    two = 6 * C2 + HID2 + C2
    vec_two = jnp.concatenate([vectors[: 6 * C2], vectors[6 * C2 + HID2 : two]]).reshape(7, C2)
    vec_hid_two = vectors[6 * C2 : 6 * C2 + HID2].reshape(1, HID2)
    wide_end = two + 7 * C3
    vec_three = jnp.concatenate([vectors[two:wide_end], vectors[wide_end + HID3 :]])
    vec_three = jnp.pad(vec_three.reshape(8, C3), ((0, 0), (0, WIDE - C3)))
    vec_hid_three = vectors[wide_end : wide_end + HID3].reshape(1, HID3)

    flips = turned.reshape(-1, 1, 1, 1)
    goal = out_grad.reshape(2 * pairs, H3, W3, C3)
    goal = jnp.where(flips, goal.transpose(0, 2, 1, 3), goal)[:, :LINES]
    goal = goal.reshape(pairs, 2, LINES, W3, C3).transpose(0, 2, 3, 1, 4)
    goal = goal.reshape(pairs, LINES, 2 * W3, C3)
    goal = jnp.pad(goal, ((0, 0), (0, 0), (0, LINE - 2 * W3), (0, WIDE - C3)))
    goal = goal.reshape(pairs, AREA, WIDE)

    result, pixel_back, near, far = run_main(
        slot_of,
        place_of,
        sizes,
        strips,
        goal,
        (vec_two, vec_hid_two, vec_three, vec_hid_three),
        pieces,
        extra,
    )
    result = result.reshape(pairs, LINES, LINE, WIDE)[:, :, : 2 * W3, :C3]
    result = result.reshape(pairs, LINES, W3, 2, C3).transpose(0, 3, 1, 2, 4)
    result = result.reshape(2 * pairs, LINES, W3, C3)
    result = jnp.pad(result, ((0, 0), (0, H3 - LINES), (0, 0), (0, 0)))
    result = jnp.where(flips, result.transpose(0, 2, 1, 3), result)

    near = near.reshape(-1, owned + extra, HALF, 128)
    far = far.reshape(near.shape)
    if paired:
        own, *parts = fold_pair(near, swap(far, 1))
        pieces = [own] + [swap(part, 2 * k + 2) for k, part in enumerate(parts)]
    else:
        pieces = list(share_out(jnp.concatenate([near, far], axis=0), "tile"))
    own, *parts = fold_tile(spot, pieces, batch_count)
    pixel_back, own = lax.optimization_barrier((pixel_back, own))
    parts = [
        lax.ppermute(part, "batch", [(i, (i + k + 1) % batch_count) for i in range(batch_count)])
        for k, part in enumerate(parts)
    ]
    returned = share_out(pixel_back, "tile").astype(f32).reshape(pixels.shape)
    returned, own = lax.optimization_barrier((returned, own))
    quarter, norm = fold_batch(spot, own, parts, owned, tile_count)
    quarters = [quarter] + [
        lax.ppermute(quarter, "batch", [(i, (i + k) % batch_count) for i in range(batch_count)])
        for k in range(1, batch_count)
    ]
    norm = share_out(norm, ("batch", "tile"))
    block_grad, left_new, right_new, master_new, weight_copy, whole_vector, clip = update(
        spot, norm, quarters, extra, master, left_stat, right_stat, left_root, right_root
    )
    clip_norm = clip[0, 0]
    share = vectors.shape[0] // tile_count
    whole_vector = whole_vector.reshape(-1)
    vec_grad = lax.dynamic_slice_in_dim(whole_vector, tile_place * share, share, 0)
    vec_moment = moment + vec_grad * vec_grad
    own_vectors = lax.dynamic_slice_in_dim(vectors, tile_place * share, share, 0)
    vec_new = own_vectors - rate_vector * vec_grad / (jnp.sqrt(vec_moment) + eps_adagrad)
    return (
        result.reshape(out_grad.shape),
        returned,
        clip_norm,
        block_grad,
        left_new,
        right_new,
        master_new,
        weight_copy,
        vec_grad,
        vec_moment,
        vec_new,
    )


def solution(mesh):
    placed = (
        P("batch", "tile", None, None, None, None),
        P("batch"),
        P(),
        P("batch", "tile", None, None, None, None, None),
        P("tile", None, None),
        P("tile", None, None),
        P("tile", None, None),
        P("tile", None, None),
        P("tile", None, None),
        P(),
        P("tile"),
    )
    return jax.shard_map(
        on_device,
        mesh=mesh,
        in_specs=placed,
        out_specs=(
            P("batch", "tile", None, None, None, None, None),
            P("batch", "tile", None, None, None, None),
            P(),
            P("tile", None, None),
            P("tile", None, None),
            P("tile", None, None),
            P("tile", None, None),
            P("tile", None, None),
            P("tile"),
            P("tile"),
            P("tile"),
        ),
        check_vma=False,
    )
```

```python
import functools

import jax
import jax.numpy as jnp
from jax import lax
from jax.experimental import pallas as pl
from jax.experimental.pallas import tpu as pltpu
from jax.sharding import PartitionSpec as P

C2 = 128
HID2 = 512
C3 = 320
HID3 = 1280
CH = 36
CW = 36
STRIPS = 4
BS = 64
SR = CH // STRIPS
H3 = CH // 2
W3 = CW // 2
LONG = 7 * CH // 9
LINES = LONG // 2
WIDE = 384
LINE = 40
AREA = LINES * LINE
STEP = 2 * LINE
STEPS = AREA // STEP
HALF = BS // 2

eps_norm = 1e-05
clip_limit = 1.0
rate_matrix = 0.3
rate_vector = 0.3
eps_adagrad = 1e-08
f32 = jnp.float32
bf16 = jnp.bfloat16

SHAPES = [(C2, HID2), (HID2, C2), (9 * C2, C3), (C3, HID3), (HID3, C3)]
USED = sum(rows // BS * (cols // BS) for rows, cols in SHAPES)
VEC_ROWS = (6 * C2 + HID2 + C2 + C3 + 6 * C3 + HID3 + C3) // 128


def extra_of(owned, groups):
    extra = -(-VEC_ROWS // HALF)
    return extra + -(owned + extra) % groups


def product(left, right):
    return jnp.dot(left, right, preferred_element_type=f32)


def product_nt(left, right):
    return lax.dot_general(left, right, (((1,), (1,)), ((), ())), preferred_element_type=f32)


def product_tn(left, right):
    return lax.dot_general(left, right, (((0,), (0,)), ((), ())), preferred_element_type=f32)


def gelu_pair(values):
    bell = jnp.exp2(values * values * (-0.5 * 1.4426950408889634))
    step = pl.reciprocal(1.0 + (0.3275911 * 0.7071067811865476) * jnp.abs(values), approx=True)
    tail = step * (
        0.5 * 0.254829592
        + step
        * (
            0.5 * -0.284496736
            + step
            * (0.5 * 1.421413741 + step * (0.5 * -1.453152027 + step * (0.5 * 1.061405429)))
        )
    )
    tail = tail * bell
    share = jnp.where(values >= 0.0, 1.0 - tail, tail)
    return (values * share, share + values * (bell * 0.3989422804014327))


def fold(values):
    chans = values.shape[-1]
    return jnp.sum(values.reshape(-1, 8, chans), axis=0)


def by_image(total):
    total = total + pltpu.roll(total, 4, 0)
    total = total + pltpu.roll(total, 2, 0)
    return jnp.sum(total, axis=1, keepdims=True)


def line(pattern):
    return jnp.concatenate([pattern] * (LINE // 8), axis=0)


def spread(pattern, chans):
    return jnp.broadcast_to(pattern, (8, chans))


def affine(values, factor, shift):
    tiles = values.reshape(-1, 8, values.shape[-1])
    return (tiles * factor + shift).reshape(values.shape)


def scaled(values, factor):
    tiles = values.reshape(-1, 8, values.shape[-1])
    return (tiles * factor).reshape(values.shape)


def from_left(values):
    return pltpu.roll(values, 2, 0)


def from_right(values):
    return pltpu.roll(values, values.shape[0] - 2, 0)


def rounded(values):
    return values.astype(bf16).astype(f32)


def widen(values):
    return jnp.concatenate([values] * (WIDE // 128), axis=-1)


def norm_terms(total, square, count):
    mean = by_image(total) / count
    scaling = lax.rsqrt(by_image(square) / count - mean * mean + eps_norm)
    return (mean, scaling)


def sweep(visit, start):
    return lax.fori_loop(0, STEPS, visit, start, unroll=True)


def step_rows(k, lines=0):
    start = k * STEP + lines * LINE
    return pl.ds(start if isinstance(k, int) else pl.multiple_of(start, LINE), STEP)


def main_kernel(
    pairs,
    strip_count,
    slots,
    extra,
    piece_count,
    slot_ref,
    place_ref,
    size_ref,
    strips_ref,
    goal_ref,
    vec_two_ref,
    vec_hid_two_ref,
    vec_three_ref,
    vec_hid_three_ref,
    *refs,
):
    inner_kernel(
        pairs,
        strip_count,
        slots,
        extra,
        slot_ref,
        place_ref,
        size_ref,
        strips_ref,
        goal_ref,
        vec_two_ref,
        vec_hid_two_ref,
        vec_three_ref,
        vec_hid_three_ref,
        refs[:piece_count],
        *refs[piece_count:],
    )


def inner_kernel(
    pairs,
    strip_count,
    slots,
    extra,
    slot_ref,
    place_ref,
    size_ref,
    strips_ref,
    goal_ref,
    vec_two_ref,
    vec_hid_two_ref,
    vec_three_ref,
    vec_hid_three_ref,
    piece_refs,
    result_ref,
    pixel_ref,
    near_ref,
    far_ref,
    gathered_ref,
    grad_ref,
    strips,
    image_ref,
    x_ref,
    inv_ref,
    col_ref,
    pool_ref,
    mix_ref,
    zed_ref,
    dx_ref,
    hid_ref,
    u_ref,
    g_ref,
    h_ref,
    dy_ref,
    patch_ref,
    dpatch_ref,
    inv3_ref,
    e_ref,
    col3_ref,
    pool3_ref,
    mix3_ref,
    dx3_ref,
    hid3_ref,
    dhid3_ref,
    u3_ref,
    g3_ref,
    h3_ref,
    dy3_ref,
    dpre_ref,
    w1_ref,
    w2_ref,
    we_ref,
    w3_ref,
    w4_ref,
    gw1_ref,
    gw2_ref,
    gwe_ref,
    gw3_ref,
    gw4_ref,
    acc_two,
    acc_hid_two,
    acc_three,
    acc_hid_three,
    flat_ref,
    in_sem,
    out_sem,
    piece_sem,
    grad_sem,
):
    pair = pl.program_id(0)
    weights = [w1_ref, w2_ref, we_ref, w3_ref, w4_ref]
    grads = [gw1_ref, gw2_ref, gwe_ref, gw3_ref, gw4_ref]

    def strip_copies(outward):
        copies = []
        for half in range(4):
            start = lax.rem(pair * 8 + strip_count - 2 + 2 * half, strip_count)
            inside = strips.at[pl.ds(2 * half, 2)]
            if outward:
                copies.append(
                    pltpu.make_async_copy(inside, pixel_ref.at[pl.ds(start, 2)], out_sem.at[half])
                )
            else:
                copies.append(
                    pltpu.make_async_copy(strips_ref.at[pl.ds(start, 2)], inside, in_sem.at[half])
                )
        return copies

    for copy in strip_copies(False):
        copy.start()

    left_half = lax.broadcasted_iota(jnp.int32, (HALF, 128), 1) < BS

    def piece_copies():
        count = slots // len(piece_refs)
        return [
            pltpu.make_async_copy(
                ref, gathered_ref.at[pl.ds(n * count, count)], piece_sem.at[n]
            )
            for n, ref in enumerate(piece_refs)
        ]

    def grad_copies():
        half = grad_ref.shape[0] // 2
        return [
            pltpu.make_async_copy(grad_ref.at[pl.ds(n * half, half)], ref, grad_sem.at[n])
            for n, ref in enumerate((near_ref, far_ref))
        ]

    def unpack():
        for copy in piece_copies():
            copy.wait()
        offset = 0
        for (rows, cols), ref in zip(SHAPES, weights):
            wide = cols // BS
            for rb in range(rows // BS):
                for cb in range(0, wide, 2):
                    number = offset + rb * wide + cb
                    first = gathered_ref[slot_ref[number]].astype(f32)
                    turned = pltpu.roll(first, BS, 1)
                    if cb + 1 < wide:
                        second = gathered_ref[slot_ref[number + 1]].astype(f32)
                        top = jnp.where(left_half, first, pltpu.roll(second, BS, 1))
                        low = jnp.where(left_half, turned, second)
                    else:
                        top = jnp.where(left_half, first, 0.0)
                        low = jnp.where(left_half, turned, 0.0)
                    place = slice(cb * BS, cb * BS + 128)
                    ref[rb * BS : rb * BS + HALF, place] = top.astype(bf16)
                    ref[rb * BS + HALF : rb * BS + BS, place] = low.astype(bf16)
            offset += rows // BS * wide
        w3_ref[C3:, :] = jnp.zeros((WIDE - C3, HID3), bf16)

    @pl.when(pair == 0)
    def _():
        for copy in piece_copies():
            copy.start()
        acc_two[...] = jnp.zeros(acc_two.shape, f32)
        acc_hid_two[...] = jnp.zeros(acc_hid_two.shape, f32)
        acc_three[...] = jnp.zeros(acc_three.shape, f32)
        acc_hid_three[...] = jnp.zeros(acc_hid_three.shape, f32)

    parity = lax.broadcasted_iota(jnp.int32, (8, 128), 0) % 2
    high, broad, turned = (
        jnp.where(parity == 0, size_ref[pair * 6 + n], size_ref[pair * 6 + 3 + n])
        for n in range(3)
    )
    count_two = (high * broad * C2).astype(f32)[:, :1]
    high3 = (high + 1) // 2
    broad3 = (broad + 1) // 2
    count_three = (high3 * broad3 * C3).astype(f32)[:, :1]
    place = lax.broadcasted_iota(jnp.int32, (LINE, 128), 0) // 2
    inside = lax.broadcasted_iota(jnp.int32, (LINE, 128), 0) < 2 * W3
    reach = []
    col_share = []
    for pc in range(2):
        column = 2 * place + pc
        reach.append(jnp.where(inside & (column < line(broad)), line(high), 0))
        edge = (column == 0) | (column == line(broad) - 1)
        col_share.append(jnp.where(edge, 0.5, 1.0 / 3.0))
    reach3 = jnp.where(inside & (place < line(broad3)), line(high3), 0)
    edge3 = (place == 0) | (place == line(broad3) - 1)
    col_share3 = jnp.where(edge3, 0.5, 1.0 / 3.0)
    flipped = jnp.concatenate([turned] * (STEP // 8), axis=0) > 0

    def row_share(row, height):
        return jnp.where((row == 0) | (row == height - 1), 0.5, 1.0 / 3.0)

    def inverse_count(row, reach, col_share, height):
        return jnp.where(row < reach, line(row_share(row, height)) * col_share, 0.0)

    gain1, bias1, scale1 = (vec_two_ref[n : n + 1] for n in range(3))
    gain2, bias2, scale2, out_bias = (vec_two_ref[n : n + 1] for n in range(3, 7))
    embed_bias, gain3, bias3, scale3 = (vec_three_ref[n : n + 1] for n in range(4))
    gain4, bias4, scale4, out_bias3 = (vec_three_ref[n : n + 1] for n in range(4, 8))

    for copy in strip_copies(False):
        copy.wait()

    zero_line = jnp.zeros((LINE, C2), f32)
    zero_line3 = jnp.zeros((LINE, WIDE), f32)
    for plane in range(4):
        col_ref[plane, 0:LINE] = zero_line
        col_ref[plane, AREA + LINE : AREA + 2 * LINE] = zero_line
        zed_ref[plane, 0:LINE] = zero_line
    col3_ref[0:LINE] = zero_line3
    col3_ref[AREA + LINE : AREA + 2 * LINE] = zero_line3

    def to_rows(within, carry):
        for spot in range(2 * STRIPS):
            image, strip = spot // STRIPS, spot % STRIPS
            start = pl.multiple_of((strip * SR + within) * LINE, LINE)
            image_ref[image, pl.ds(start, CW)] = strips[spot, within].astype(f32)
        return carry

    lax.fori_loop(0, SR, to_rows, 0)

    def plane_places(image, flat, r):
        for pr in range(2):
            for pc in range(2):
                line_place = pl.ds(r * LINE + image, W3, stride=2)
                if flat:
                    there = pl.ds((2 * r + pr) * LINE + pc, W3, stride=2)
                else:
                    there = pl.ds(pc * LINE + 2 * r + pr, W3, stride=2 * LINE)
                yield (pr * 2 + pc, line_place, there)

    def each_image(visit):
        for image in range(2):
            way = size_ref[pair * 6 + 3 * image + 2]
            for flat in (True, False):

                @pl.when(way == (0 if flat else 1))
                def _():
                    def one(r, carry):
                        for plane, line_place, there in plane_places(image, flat, r):
                            visit(image, plane, line_place, there)
                        return carry

                    lax.fori_loop(0, LINES, one, 0)

    def take_in(image, plane, line_place, there):
        x_ref[plane, line_place] = image_ref[image, there]

    each_image(take_in)

    def arrange(k, carry):
        total, square = carry
        rows = step_rows(k)
        for plane in range(4):
            pr, pc = plane // 2, plane % 2
            share = jnp.concatenate(
                [
                    inverse_count(4 * k + 2 * n + pr, reach[pc], col_share[pc], high)
                    for n in range(2)
                ],
                axis=0,
            )
            inv_ref[plane, rows] = share
            values = jnp.where(share > 0.0, x_ref[plane, rows], 0.0)
            x_ref[plane, rows] = values
            total = total + fold(values)
            square = square + fold(values * values)
        inv3_ref[rows] = jnp.concatenate(
            [inverse_count(2 * k + n, reach3, col_share3, high3) for n in range(2)], axis=0
        )
        return (total, square)

    nothing = jnp.zeros((8, C2), f32)
    nothing3 = jnp.zeros((8, WIDE), f32)
    total, square = sweep(arrange, (nothing, nothing))
    mean1, scaling1 = norm_terms(total, square, count_two)
    factor1 = scaling1 * gain1
    shift1 = bias1 - mean1 * scaling1 * gain1

    def window_cols(k, carry):
        rows = step_rows(k)
        for pr in range(2):
            masked = []
            for pc in range(2):
                plane = pr * 2 + pc
                normal = rounded(affine(x_ref[plane, rows], factor1, shift1))
                masked.append(jnp.where(inv_ref[plane, rows] > 0.0, normal, 0.0))
            both = masked[0] + masked[1]
            col_ref[pr * 2, step_rows(k, 1)] = both + from_left(masked[1])
            col_ref[pr * 2 + 1, step_rows(k, 1)] = both + from_right(masked[0])
        return carry

    sweep(window_cols, 0)

    def row_windows(pc, k):
        both = col_ref[pc, step_rows(k, 1)] + col_ref[2 + pc, step_rows(k, 1)]
        return (both + col_ref[2 + pc, step_rows(k)], both + col_ref[pc, step_rows(k, 2)])

    def mix(k, carry):
        total, square = carry
        rows = step_rows(k)
        for pc in range(2):
            windows = row_windows(pc, k)
            for pr in range(2):
                plane = pr * 2 + pc
                values = x_ref[plane, rows]
                share = inv_ref[plane, rows]
                pooled = windows[pr] * share - rounded(affine(values, factor1, shift1))
                pooled = jnp.where(share > 0.0, pooled, 0.0)
                mixed = values + scale1 * pooled
                pool_ref[plane, rows] = pooled
                mix_ref[plane, rows] = mixed
                total = total + fold(mixed)
                square = square + fold(mixed * mixed)
        return (total, square)

    total, square = sweep(mix, (nothing, nothing))
    pl.when(pair == 0)(unpack)
    mean2, scaling2 = norm_terms(total, square, count_two)
    factor2 = scaling2 * gain2
    shift2 = bias2 - mean2 * scaling2 * gain2

    def plane_rows(plane):
        return pl.ds(pl.multiple_of(plane * AREA, AREA), AREA)

    def branch(plane, carry):
        mixed = mix_ref[plane]
        low = affine(mixed, factor2, shift2).astype(bf16)
        h_ref[plane_rows(plane)] = low
        hid_ref[...] = product(low, w1_ref[...])

        def activate(k, carry):
            rows = step_rows(k)
            flat = pl.ds(pl.multiple_of(plane * AREA + k * STEP, STEP), STEP)
            for at in range(0, HID2, 128):
                lanes = slice(at, at + 128)
                active, slope = gelu_pair(hid_ref[rows, lanes] + vec_hid_two_ref[:, lanes])
                u_ref[flat, lanes] = active.astype(bf16)
                g_ref[flat, lanes] = slope.astype(bf16)
            return carry

        sweep(activate, 0)
        out = product(u_ref[plane_rows(plane)], w2_ref[...]) + out_bias
        zed = jnp.where(inv_ref[plane] > 0.0, mixed + scale2 * out, 0.0)
        zed_ref[plane, LINE : LINE + AREA] = rounded(zed)
        return carry

    lax.fori_loop(0, 4, branch, 0)

    def patches(k, carry):
        rows = step_rows(k)
        taps = []
        for ky in range(3):
            pr = (0 if ky == 1 else 1) * 2
            source = step_rows(k, 0 if ky == 0 else 1)
            even = zed_ref[pr, source]
            odd = zed_ref[pr + 1, source]
            taps.append((from_left(odd), even, odd))
        for ky in range(3):
            for kx in range(3):
                at = (3 * ky + kx) * C2
                tap = taps[ky][kx]
                if ky != kx:
                    tap = jnp.where(flipped, taps[kx][ky], tap)
                patch_ref[rows, at : at + C2] = tap.astype(bf16)
        return carry

    sweep(patches, 0)
    e_ref[...] = product(patch_ref[...], we_ref[...])

    def embed(k, carry):
        total, square = carry
        rows = step_rows(k)
        out = jnp.where(widen(inv3_ref[rows]) > 0.0, e_ref[rows] + embed_bias, 0.0)
        e_ref[rows] = out
        return (total + fold(out), square + fold(out * out))

    total, square = sweep(embed, (nothing3, nothing3))
    mean3, scaling3 = norm_terms(total, square, count_three)
    factor3 = scaling3 * gain3
    shift3 = bias3 - mean3 * scaling3 * gain3

    def window_cols3(k, carry):
        rows = step_rows(k)
        normal = rounded(affine(e_ref[rows], factor3, shift3))
        masked = jnp.where(widen(inv3_ref[rows]) > 0.0, normal, 0.0)
        col3_ref[step_rows(k, 1)] = masked + from_left(masked) + from_right(masked)
        return carry

    sweep(window_cols3, 0)

    def row_windows3(k):
        return col3_ref[step_rows(k)] + col3_ref[step_rows(k, 1)] + col3_ref[step_rows(k, 2)]

    def mix3(k, carry):
        total, square = carry
        rows = step_rows(k)
        values = e_ref[rows]
        share = widen(inv3_ref[rows])
        pooled = row_windows3(k) * share - rounded(affine(values, factor3, shift3))
        pooled = jnp.where(share > 0.0, pooled, 0.0)
        mixed = values + scale3 * pooled
        pool3_ref[rows] = pooled
        mix3_ref[rows] = mixed
        return (total + fold(mixed), square + fold(mixed * mixed))

    total, square = sweep(mix3, (nothing3, nothing3))
    mean4, scaling4 = norm_terms(total, square, count_three)
    factor4 = scaling4 * gain4
    shift4 = bias4 - mean4 * scaling4 * gain4
    normal4 = (spread(scaling4, WIDE), spread(-mean4 * scaling4, WIDE))

    def prepare3(k, d_bias):
        rows = step_rows(k)
        h3_ref[rows] = affine(mix3_ref[rows], factor4, shift4).astype(bf16)
        goal = goal_ref[0, rows].astype(f32)
        goal = jnp.where(widen(inv3_ref[rows]) > 0.0, goal, 0.0)
        low_goal = (scale4 * goal).astype(bf16)
        dy3_ref[rows] = low_goal
        return d_bias + fold(low_goal.astype(f32))

    acc_three[7] += sweep(prepare3, nothing3)
    hid3_ref[...] = product(h3_ref[...], w3_ref[...])
    dhid3_ref[...] = product_nt(dy3_ref[...], w4_ref[...])

    def activate3(k, sums):
        rows = step_rows(k)
        new = []
        for n, at in enumerate(range(0, HID3, 128)):
            lanes = slice(at, at + 128)
            active, slope = gelu_pair(hid3_ref[rows, lanes] + vec_hid_three_ref[:, lanes])
            u3_ref[rows, lanes] = active.astype(bf16)
            low = (slope * dhid3_ref[rows, lanes]).astype(bf16)
            g3_ref[rows, lanes] = low
            new.append(sums[n] + fold(low.astype(f32)))
        return tuple(new)

    sums = sweep(activate3, (nothing,) * (HID3 // 128))
    for n, value in enumerate(sums):
        acc_hid_three[:, n * 128 : n * 128 + 128] += value

    def keep(ref, value):
        if pairs == 1:
            ref[...] = value
        else:

            @pl.when(pair == 0)
            def _():
                ref[...] = value

            @pl.when(pair > 0)
            def _():
                ref[...] += value

    result_ref[0] = product(u3_ref[...], w4_ref[...])
    dx3_ref[...] = product_nt(g3_ref[...], w3_ref[...])
    keep(gw3_ref, product_tn(h3_ref[...], g3_ref[...]))
    keep(gw4_ref, product_tn(u3_ref[...], dy3_ref[...]))

    def finish3(k, carry):
        d_scale, d_shift, d_gain = carry
        rows = step_rows(k)
        valid = widen(inv3_ref[rows]) > 0.0
        mixed = mix3_ref[rows]
        out = jnp.where(valid, result_ref[0, rows] + out_bias3, 0.0)
        result_ref[0, rows] = mixed + scale4 * out
        d_scale = d_scale + fold(out * goal_ref[0, rows].astype(f32))
        d_low = dx3_ref[rows]
        normal = affine(mixed, *normal4)
        return (d_scale, d_shift + fold(d_low), d_gain + fold(d_low * normal))

    d_scale, d_shift, d_gain = sweep(finish3, (nothing3, nothing3, nothing3))
    acc_three[6] += d_scale
    acc_three[5] += d_shift
    acc_three[4] += d_gain
    mean_shift = by_image(d_shift * gain4) / count_three
    mean_gain = by_image(d_gain * gain4) / count_three
    back_gain4 = scaling4 * gain4
    back_mean4 = spread(-scaling4 * mean_shift, WIDE)
    back_normal4 = spread(scaling4 * mean_gain, WIDE)

    def unmix3(k, d_scale):
        rows = step_rows(k)
        share = widen(inv3_ref[rows])
        valid = share > 0.0
        normal = affine(mix3_ref[rows], *normal4)
        back = affine(dx3_ref[rows], back_gain4, back_mean4) - scaled(normal, back_normal4)
        d_mixed = jnp.where(valid, back + goal_ref[0, rows].astype(f32), 0.0)
        dx3_ref[rows] = d_mixed
        d_scale = d_scale + fold(pool3_ref[rows] * d_mixed)
        weighted = scale3 * d_mixed * share
        col3_ref[step_rows(k, 1)] = weighted + from_left(weighted) + from_right(weighted)
        return d_scale

    acc_three[3] += sweep(unmix3, nothing3)
    normal3 = (spread(scaling3, WIDE), spread(-mean3 * scaling3, WIDE))

    def unpool3(k, carry):
        d_shift, d_gain = carry
        rows = step_rows(k)
        valid = widen(inv3_ref[rows]) > 0.0
        d_normal = jnp.where(valid, row_windows3(k) - scale3 * dx3_ref[rows], 0.0)
        pool3_ref[rows] = d_normal
        normal = affine(e_ref[rows], *normal3)
        return (d_shift + fold(d_normal), d_gain + fold(d_normal * normal))

    d_shift, d_gain = sweep(unpool3, (nothing3, nothing3))
    acc_three[2] += d_shift
    acc_three[1] += d_gain
    mean_shift = by_image(d_shift * gain3) / count_three
    mean_gain = by_image(d_gain * gain3) / count_three
    back_gain3 = scaling3 * gain3
    back_mean3 = spread(-scaling3 * mean_shift, WIDE)
    back_normal3 = spread(scaling3 * mean_gain, WIDE)

    def unnorm3(k, d_bias):
        rows = step_rows(k)
        valid = widen(inv3_ref[rows]) > 0.0
        normal = affine(e_ref[rows], *normal3)
        back = affine(pool3_ref[rows], back_gain3, back_mean3) - scaled(normal, back_normal3)
        low = jnp.where(valid, dx3_ref[rows] + back, 0.0).astype(bf16)
        dpre_ref[rows] = low
        return d_bias + fold(low.astype(f32))

    acc_three[0] += sweep(unnorm3, nothing3)
    keep(gwe_ref, product_tn(patch_ref[...], dpre_ref[...]))
    dpatch_ref[0:AREA] = product_nt(dpre_ref[...], we_ref[...])
    dpatch_ref[AREA : AREA + LINE] = jnp.zeros((LINE, 9 * C2), f32)

    def gather_back(k, carry):
        rows = step_rows(k)

        def tap(ky, kx, source):
            at = (3 * ky + kx) * C2
            value = dpatch_ref[source, at : at + C2]
            if ky != kx:
                at = (3 * kx + ky) * C2
                value = jnp.where(flipped, dpatch_ref[source, at : at + C2], value)
            return value

        sources = []
        for ky in range(3):
            source = step_rows(k, 1 if ky == 0 else 0)
            sources.append(
                (tap(ky, 1, source), tap(ky, 2, source) + from_right(tap(ky, 0, source)))
            )
        for pc in range(2):
            for pr, value in ((0, sources[1][pc]), (1, sources[2][pc] + sources[0][pc])):
                plane = pr * 2 + pc
                valid = inv_ref[plane, rows] > 0.0
                zed_ref[plane, rows] = jnp.where(valid, rounded(value), 0.0)
        return carry

    sweep(gather_back, 0)

    normal2 = (spread(scaling2, C2), spread(-mean2 * scaling2, C2))

    def unbranch(plane, carry):
        d_out_bias, d_shift, d_gain, sums = carry
        flat = plane_rows(plane)
        low_goal = (scale2 * zed_ref[plane, 0:AREA]).astype(bf16)
        dy_ref[flat] = low_goal
        hid_ref[...] = product_nt(low_goal, w2_ref[...])

        def slopes(k, sums):
            rows = step_rows(k)
            part = pl.ds(pl.multiple_of(plane * AREA + k * STEP, STEP), STEP)
            new = []
            for n, at in enumerate(range(0, HID2, 128)):
                lanes = slice(at, at + 128)
                low = (g_ref[part, lanes].astype(f32) * hid_ref[rows, lanes]).astype(bf16)
                g_ref[part, lanes] = low
                new.append(sums[n] + fold(low.astype(f32)))
            return tuple(new)

        sums = sweep(slopes, sums)
        d_low = product_nt(g_ref[flat], w1_ref[...])
        dx_ref[plane] = d_low
        normal = affine(mix_ref[plane], *normal2)
        return (
            d_out_bias + fold(low_goal.astype(f32)),
            d_shift + fold(d_low),
            d_gain + fold(d_low * normal),
            sums,
        )

    d_out_bias, d_shift, d_gain, sums = lax.fori_loop(
        0, 4, unbranch, (nothing, nothing, nothing, (nothing,) * (HID2 // 128))
    )
    for n, value in enumerate(sums):
        acc_hid_two[:, n * 128 : n * 128 + 128] += value
    acc_two[6] += d_out_bias
    acc_two[4] += d_shift
    acc_two[3] += d_gain
    mean_shift = by_image(d_shift * gain2) / count_two
    mean_gain = by_image(d_gain * gain2) / count_two
    keep(gw1_ref, product_tn(h_ref[...], g_ref[...]))
    new_gw2 = product_tn(dy_ref[...], u_ref[...]).T
    keep(gw2_ref, new_gw2)
    d_scale = fold(w2_ref[...].astype(f32) * new_gw2) + out_bias * d_out_bias
    acc_two[5] += d_scale / scale2

    back_gain2 = scaling2 * gain2
    back_mean2 = spread(-scaling2 * mean_shift, C2)
    back_normal2 = spread(scaling2 * mean_gain, C2)

    def unmix(k, d_scale):
        rows = step_rows(k)
        for pr in range(2):
            weighted = []
            for pc in range(2):
                plane = pr * 2 + pc
                share = inv_ref[plane, rows]
                normal = affine(mix_ref[plane, rows], *normal2)
                back = affine(dx_ref[plane, rows], back_gain2, back_mean2)
                back = back - scaled(normal, back_normal2)
                d_mixed = jnp.where(share > 0.0, zed_ref[plane, rows] + back, 0.0)
                dx_ref[plane, rows] = d_mixed
                d_scale = d_scale + fold(pool_ref[plane, rows] * d_mixed)
                weighted.append(scale1 * d_mixed * share)
            both = weighted[0] + weighted[1]
            col_ref[pr * 2, step_rows(k, 1)] = both + from_left(weighted[1])
            col_ref[pr * 2 + 1, step_rows(k, 1)] = both + from_right(weighted[0])
        return d_scale

    acc_two[2] += sweep(unmix, nothing)
    normal1 = (spread(scaling1, C2), spread(-mean1 * scaling1, C2))

    def unpool(k, carry):
        d_shift, d_gain = carry
        rows = step_rows(k)
        for pc in range(2):
            windows = row_windows(pc, k)
            for pr in range(2):
                plane = pr * 2 + pc
                valid = inv_ref[plane, rows] > 0.0
                d_normal = windows[pr] - scale1 * dx_ref[plane, rows]
                d_normal = jnp.where(valid, d_normal, 0.0)
                pool_ref[plane, rows] = d_normal
                normal = affine(x_ref[plane, rows], *normal1)
                d_shift = d_shift + fold(d_normal)
                d_gain = d_gain + fold(d_normal * normal)
        return (d_shift, d_gain)

    d_shift, d_gain = sweep(unpool, (nothing, nothing))
    acc_two[1] += d_shift
    acc_two[0] += d_gain
    mean_shift = by_image(d_shift * gain1) / count_two
    mean_gain = by_image(d_gain * gain1) / count_two
    back_gain1 = scaling1 * gain1
    back_mean1 = spread(-scaling1 * mean_shift, C2)
    back_normal1 = spread(scaling1 * mean_gain, C2)

    def unnorm(k, carry):
        rows = step_rows(k)
        for plane in range(4):
            normal = affine(x_ref[plane, rows], *normal1)
            back = affine(pool_ref[plane, rows], back_gain1, back_mean1)
            back = back - scaled(normal, back_normal1)
            valid = inv_ref[plane, rows] > 0.0
            dx_ref[plane, rows] = jnp.where(valid, dx_ref[plane, rows] + back, 0.0)
        return carry

    sweep(unnorm, 0)

    def give_back(image, plane, line_place, there):
        image_ref[image, there] = dx_ref[plane, line_place]

    image_ref[...] = jnp.zeros(image_ref.shape, f32)
    each_image(give_back)

    def from_rows(within, carry):
        for spot in range(2 * STRIPS):
            image, strip = spot // STRIPS, spot % STRIPS
            start = pl.multiple_of((strip * SR + within) * LINE, LINE)
            strips[spot, within] = image_ref[image, pl.ds(start, CW)].astype(bf16)
        return carry

    lax.fori_loop(0, SR, from_rows, 0)
    for copy in strip_copies(True):
        copy.start()

    @pl.when(pair == pairs - 1)
    def _():
        offset = 0
        for (rows, cols), ref in zip(SHAPES, grads):
            wide = cols // BS
            for rb in range(rows // BS):
                for cb in range(0, wide, 2):
                    number = offset + rb * wide + cb
                    at = slice(cb * BS, cb * BS + 128)
                    top = ref[rb * BS : rb * BS + HALF, at]
                    low = ref[rb * BS + HALF : rb * BS + BS, at]
                    grad_ref[place_ref[number]] = jnp.where(
                        left_half, top, pltpu.roll(low, BS, 1)
                    ).astype(bf16)
                    if cb + 1 < wide:
                        grad_ref[place_ref[number + 1]] = jnp.where(
                            left_half, pltpu.roll(top, BS, 1), low
                        ).astype(bf16)
            offset += rows // BS * wide

        def filler(number, carry):
            grad_ref[place_ref[number]] = jnp.zeros((HALF, 128), bf16)
            return carry

        lax.fori_loop(USED, slots, filler, 0)

        flat_ref[...] = jnp.zeros(flat_ref.shape, f32)

        def put(at, total, length):
            if at % 128:
                room = jnp.zeros((8, 128), f32)
                if total.shape[1] < length + BS:
                    total = jnp.concatenate([total, room], axis=1)
                total = pltpu.roll(total, BS, 1)
            whole = jnp.sum(total, axis=0, keepdims=True)
            done = -(at % 128)
            row = at // 128
            lane = 0
            while done < length:
                first = max(0, -done)
                last = min(128, length - done)
                flat_ref[row : row + 1, first:last] = whole[:, lane + first : lane + last]
                done += 128
                lane += 128
                row += 1

        at = 0
        for n in range(6):
            put(at, acc_two[n], C2)
            at += C2
        put(at, acc_hid_two[...], HID2)
        at += HID2
        put(at, acc_two[6], C2)
        at += C2
        for n in range(7):
            put(at, acc_three[n], C3)
            at += C3
        put(at, acc_hid_three[...], HID3)
        at += HID3
        put(at, acc_three[7], C3)
        packed = flat_ref[...].astype(bf16)
        stride = slots // strip_count + extra
        for n in range(extra):
            piece = packed[n * HALF : (n + 1) * HALF]

            def leave(target, carry):
                grad_ref[target * stride + stride - extra + n] = piece
                return carry

            lax.fori_loop(0, strip_count, leave, 0)
        for copy in grad_copies():
            copy.start()
        for copy in grad_copies():
            copy.wait()

    for copy in strip_copies(True):
        copy.wait()


def run_main(slot_of, place_of, sizes, strips, goal, vectors, pieces, extra):
    strip_count = strips.shape[0]
    pairs = goal.shape[0]
    slots = sum(piece.shape[0] for piece in pieces)
    rows_out = slots + extra * strip_count

    def whole(shape):
        return pl.BlockSpec(shape, lambda t: (0,) * len(shape), pipeline_mode=pl.Buffered(1))

    smem = pl.BlockSpec(memory_space=pltpu.SMEM)
    anywhere = pl.BlockSpec(memory_space=pltpu.HBM)
    plane_f32 = pltpu.VMEM((4, AREA, C2), f32)
    wide_f32 = pltpu.VMEM((AREA, WIDE), f32)
    wide_bf16 = pltpu.VMEM((AREA, WIDE), bf16)
    scratch = [
        pltpu.VMEM((slots, HALF, 128), bf16),
        pltpu.VMEM((rows_out, HALF, 128), bf16),
        pltpu.VMEM((2 * STRIPS, SR, CW, C2), bf16),
        pltpu.VMEM((2, CH * LINE, C2), f32),
        plane_f32,
        plane_f32,
        pltpu.VMEM((4, AREA + 2 * LINE, C2), f32),
        plane_f32,
        plane_f32,
        pltpu.VMEM((4, AREA + LINE, C2), f32),
        plane_f32,
        pltpu.VMEM((AREA, HID2), f32),
        pltpu.VMEM((4 * AREA, HID2), bf16),
        pltpu.VMEM((4 * AREA, HID2), bf16),
        pltpu.VMEM((4 * AREA, C2), bf16),
        pltpu.VMEM((4 * AREA, C2), bf16),
        pltpu.VMEM((AREA, 9 * C2), bf16),
        pltpu.VMEM((AREA + LINE, 9 * C2), f32),
        pltpu.VMEM((AREA, 128), f32),
        wide_f32,
        pltpu.VMEM((AREA + 2 * LINE, WIDE), f32),
        wide_f32,
        wide_f32,
        wide_f32,
        pltpu.VMEM((AREA, HID3), f32),
        pltpu.VMEM((AREA, HID3), f32),
        pltpu.VMEM((AREA, HID3), bf16),
        pltpu.VMEM((AREA, HID3), bf16),
        wide_bf16,
        wide_bf16,
        wide_bf16,
        pltpu.VMEM((C2, HID2), bf16),
        pltpu.VMEM((HID2, C2), bf16),
        pltpu.VMEM((9 * C2, WIDE), bf16),
        pltpu.VMEM((WIDE, HID3), bf16),
        pltpu.VMEM((HID3, WIDE), bf16),
        pltpu.VMEM((C2, HID2), f32),
        pltpu.VMEM((HID2, C2), f32),
        pltpu.VMEM((9 * C2, WIDE), f32),
        pltpu.VMEM((WIDE, HID3), f32),
        pltpu.VMEM((HID3, WIDE), f32),
        pltpu.VMEM((7, 8, C2), f32),
        pltpu.VMEM((8, HID2), f32),
        pltpu.VMEM((8, 8, WIDE), f32),
        pltpu.VMEM((8, HID3), f32),
        pltpu.VMEM((extra * HALF, 128), f32),
        pltpu.SemaphoreType.DMA((4,)),
        pltpu.SemaphoreType.DMA((4,)),
        pltpu.SemaphoreType.DMA((len(pieces),)),
        pltpu.SemaphoreType.DMA((2,)),
    ]
    return pl.pallas_call(
        functools.partial(main_kernel, pairs, strip_count, slots, extra, len(pieces)),
        grid=(pairs,),
        in_specs=[
            smem,
            smem,
            smem,
            anywhere,
            pl.BlockSpec((1,) + goal.shape[1:], lambda t: (t, 0, 0)),
        ]
        + [whole(vector.shape) for vector in vectors]
        + [anywhere] * len(pieces),
        out_specs=[
            pl.BlockSpec((1, AREA, WIDE), lambda t: (t, 0, 0)),
            anywhere,
            anywhere,
            anywhere,
        ],
        out_shape=[
            jax.ShapeDtypeStruct((pairs, AREA, WIDE), f32),
            jax.ShapeDtypeStruct(strips.shape, bf16),
            jax.ShapeDtypeStruct((rows_out // 2, HALF, 128), bf16),
            jax.ShapeDtypeStruct((rows_out // 2, HALF, 128), bf16),
        ],
        scratch_shapes=scratch,
        compiler_params=pltpu.CompilerParams(
            vmem_limit_bytes=60 * 1024 * 1024, fuse_transposed_lhs_in_matmul=True
        ),
        name="blocks",
    )(slot_of, place_of, sizes, strips, goal, *vectors, *pieces)


def pack_kernel(master_ref, dense_ref):
    values = master_ref[...]
    dense_ref[...] = jnp.concatenate([values[:, :HALF], values[:, HALF:]], axis=2).astype(bf16)


def pack(master):
    owned = master.shape[0]
    return pl.pallas_call(
        pack_kernel,
        out_shape=jax.ShapeDtypeStruct((owned, HALF, 2 * BS), bf16),
        name="pack",
    )(master)


def copy_all(sources, targets, sems, first=0):
    return [
        pltpu.make_async_copy(source, target, sems.at[first + n])
        for n, (source, target) in enumerate(zip(sources, targets))
    ]


def fold_pair_kernel(near_hbm, got_hbm, *refs):
    groups = near_hbm.shape[0]
    out_hbm, (near_ref, got_ref, own_ref, part_ref, in_sem, out_sem) = refs[:groups], refs[groups:]
    copies_in = [
        copy_all(
            [near_hbm.at[n], got_hbm.at[n]], [near_ref.at[n], got_ref.at[n]], in_sem, 2 * n
        )
        for n in range(groups)
    ]
    copies_out = copy_all(
        [own_ref] + [part_ref.at[n] for n in range(groups - 1)], out_hbm, out_sem
    )
    order = list(range(1, groups)) + [0]
    for n in order:
        for copy in copies_in[n]:
            copy.start()
    for n in order:
        for copy in copies_in[n]:
            copy.wait()
        total = near_ref[n].astype(f32) + got_ref[n].astype(f32)
        if n == 0:
            own_ref[...] = total
        else:
            part_ref[n - 1] = total.astype(bf16)
        copies_out[n].start()
    for copy in copies_out:
        copy.wait()


HBM = pl.BlockSpec(memory_space=pltpu.HBM)
SMEM = pl.BlockSpec(memory_space=pltpu.SMEM)
ROOMY = pltpu.CompilerParams(vmem_limit_bytes=48 * 1024 * 1024)


def fold_pair(near, got):
    groups = near.shape[0]
    part = jax.ShapeDtypeStruct(near.shape[1:], bf16)
    own = jax.ShapeDtypeStruct(near.shape[1:], f32)
    return pl.pallas_call(
        fold_pair_kernel,
        in_specs=[HBM, HBM],
        out_specs=[HBM] * groups,
        out_shape=[own] + [part] * (groups - 1),
        scratch_shapes=[
            pltpu.VMEM(near.shape, bf16),
            pltpu.VMEM(near.shape, bf16),
            pltpu.VMEM(own.shape, f32),
            pltpu.VMEM((groups - 1,) + own.shape, bf16),
            pltpu.SemaphoreType.DMA((2 * groups,)),
            pltpu.SemaphoreType.DMA((groups,)),
        ],
        compiler_params=ROOMY,
        name="fold_pair",
    )(near, got)


def fold_tile_kernel(pieces, spot_ref, *refs):
    piece_hbm, refs = refs[:pieces], refs[pieces:]
    piece_refs, (in_sem, out_sem) = refs[-pieces - 2 : -2], refs[-2:]
    groups = (len(refs) - pieces - 2) // 2
    out_hbm, out_refs = refs[:groups], refs[groups : 2 * groups]
    share = out_refs[0].shape[0]

    def quarter(k):
        return pl.ds(lax.rem(spot_ref[0] + k, groups) * share, share)

    copies_in = [
        copy_all(
            [ref.at[quarter(k)] for ref in piece_hbm],
            [ref.at[k] for ref in piece_refs],
            in_sem,
            k * pieces,
        )
        for k in range(groups)
    ]
    copies_out = copy_all(out_refs, out_hbm, out_sem)
    order = list(range(1, groups)) + [0]
    for k in order:
        for copy in copies_in[k]:
            copy.start()
    for k in order:
        for copy in copies_in[k]:
            copy.wait()
        total = piece_refs[0][k].astype(f32)
        for ref in piece_refs[1:]:
            total = total + ref[k].astype(f32)
        out_refs[k][...] = total.astype(out_refs[k].dtype)
        copies_out[k].start()
    for copy in copies_out:
        copy.wait()


def fold_tile(spot, pieces, groups):
    share = pieces[0].shape[0] // groups
    shape = (share,) + pieces[0].shape[1:]
    types = [f32] + [bf16] * (groups - 1)
    return pl.pallas_call(
        functools.partial(fold_tile_kernel, len(pieces)),
        in_specs=[SMEM] + [HBM] * len(pieces),
        out_specs=[HBM] * groups,
        out_shape=[jax.ShapeDtypeStruct(shape, kind) for kind in types],
        scratch_shapes=[pltpu.VMEM(shape, kind) for kind in types]
        + [pltpu.VMEM((groups,) + shape, piece.dtype) for piece in pieces]
        + [
            pltpu.SemaphoreType.DMA((groups * len(pieces),)),
            pltpu.SemaphoreType.DMA((groups,)),
        ],
        compiler_params=ROOMY,
        name="fold_tile",
    )(spot, *pieces)


def fold_batch_kernel(owned, vector_weight, parts, spot_ref, *refs):
    part_hbm, refs = refs[:parts], refs[parts:]
    (total_ref, norm_ref), part_refs, sem = refs[:2], refs[2:-1], refs[-1]
    copies = copy_all(part_hbm, part_refs, sem)
    for copy in copies:
        copy.start()
    for copy in copies:
        copy.wait()
    share = total_ref.shape[0]
    square = jnp.zeros((8, 128), f32)
    for n in range(share):
        total = part_refs[0][n].astype(f32)
        for ref in part_refs[1:]:
            total = total + ref[n].astype(f32)
        total_ref[n] = total.astype(bf16)
        weight = jnp.where(spot_ref[0] * share + n < owned, 1.0, vector_weight)
        square = square + weight * fold(total * total)
    square = jnp.sum(jnp.sum(square, axis=1, keepdims=True), axis=0, keepdims=True)
    norm_ref[...] = jnp.broadcast_to(square[None], norm_ref.shape)


def fold_batch(spot, parts, owned, tile_count):
    count = tile_count * len(parts)
    return pl.pallas_call(
        functools.partial(fold_batch_kernel, owned, 1.0 / tile_count, len(parts)),
        in_specs=[SMEM] + [HBM] * len(parts),
        out_shape=[
            jax.ShapeDtypeStruct(parts[0].shape, bf16),
            jax.ShapeDtypeStruct((count, 1, 128), f32),
        ],
        scratch_shapes=[pltpu.VMEM(part.shape, part.dtype) for part in parts]
        + [pltpu.SemaphoreType.DMA((len(parts),))],
        name="fold_batch",
    )(spot, *parts)


def update_kernel(owned, groups, spot_ref, norm_hbm, *refs):
    quarter_hbm, refs = refs[:groups], refs[groups:]
    stat_hbm, out_hbm, (vector_ref, clip_ref), refs = refs[:5], refs[5:10], refs[10:12], refs[12:]
    norm_ref, refs = refs[0], refs[1:]
    quarters, refs = refs[:groups], refs[groups:]
    stat_refs, out_refs, (in_sem, out_sem, early_sem) = refs[:5], refs[5:10], refs[10:]
    master_ref, left_stat_ref, right_stat_ref, left_root_ref, right_root_ref = stat_refs
    grad_ref, left_ref, right_ref, new_ref, copy_ref = out_refs
    share = quarters[0].shape[0]
    part = 7
    early = copy_all([norm_hbm, *quarter_hbm], [norm_ref, *quarters], early_sem)
    for copy in early:
        copy.start()
    spans = [pl.ds(first, min(part, owned - first)) for first in range(0, owned, part)]
    copies_in = [
        copy_all(
            [ref.at[span] for ref in stat_hbm],
            [ref.at[span] for ref in stat_refs],
            in_sem,
            5 * n,
        )
        for n, span in enumerate(spans)
    ]
    copies_out = [
        copy_all(
            [ref.at[span] for ref in out_refs],
            [ref.at[span] for ref in out_hbm],
            out_sem,
            5 * n,
        )
        for n, span in enumerate(spans)
    ]
    for copies in copies_in:
        for copy in copies:
            copy.start()
    for copy in early:
        copy.wait()
    norm = jnp.sqrt(jnp.sum(norm_ref[...], axis=0))
    factor = jnp.minimum(1.0, clip_limit / norm)

    def summed(number):
        source = number // share
        local = number - source * share
        turn = lax.rem(spot_ref[0] - source + groups, groups)
        value = quarters[0][local].astype(f32)
        for k in range(1, groups):
            value = jnp.where(turn == k, quarters[k][local].astype(f32), value)
        return value * factor

    clip_ref[...] = norm
    for n in range(vector_ref.shape[0]):
        vector_ref[n] = summed(owned + n)
    for span, arriving, leaving in zip(spans, copies_in, copies_out):
        for copy in arriving:
            copy.wait()
        for n in range(span.start, span.start + span.size):
            dense = summed(n)
            grad = jnp.concatenate([dense[:, :BS], dense[:, BS:]], axis=0)
            grad_ref[n] = grad
            low = grad.astype(bf16)
            left_ref[n] = 0.5 * left_stat_ref[n] + 0.5 * product_nt(low, low)
            right_ref[n] = 0.5 * right_stat_ref[n] + 0.5 * product_tn(low, low)
            stepped = product(left_root_ref[n].astype(bf16), low).astype(bf16)
            stepped = product(stepped, right_root_ref[n].astype(bf16))
            new = master_ref[n] - rate_matrix * stepped
            new_ref[n] = new
            copy_ref[n] = new.astype(bf16)
        for copy in leaving:
            copy.start()
    for leaving in copies_out:
        for copy in leaving:
            copy.wait()


def update(spot, norm, quarters, extra, master, *stats):
    owned = master.shape[0]
    groups = len(quarters)
    types = [f32] * 4 + [bf16]
    steps = -(-owned // 7)
    vmem = pl.BlockSpec(memory_space=pltpu.VMEM)
    return pl.pallas_call(
        functools.partial(update_kernel, owned, groups),
        in_specs=[SMEM] + [HBM] * (groups + 6),
        out_specs=[HBM] * 5 + [vmem] * 2,
        out_shape=[jax.ShapeDtypeStruct(master.shape, kind) for kind in types]
        + [
            jax.ShapeDtypeStruct((extra, HALF, 128), f32),
            jax.ShapeDtypeStruct((1, 128), f32),
        ],
        scratch_shapes=[pltpu.VMEM(norm.shape, f32)]
        + [pltpu.VMEM(quarter.shape, bf16) for quarter in quarters]
        + [pltpu.VMEM(master.shape, f32)] * 5
        + [pltpu.VMEM(master.shape, kind) for kind in types]
        + [
            pltpu.SemaphoreType.DMA((5 * steps,)),
            pltpu.SemaphoreType.DMA((5 * steps,)),
            pltpu.SemaphoreType.DMA((groups + 1,)),
        ],
        compiler_params=ROOMY,
        name="update",
    )(spot, norm, *quarters, master, *stats)


def share_out(pieces, axis):
    return lax.all_to_all(pieces, axis, split_axis=0, concat_axis=0, tiled=True)


def swap(piece, distance):
    count = lax.axis_size("tile")
    return lax.ppermute(piece, "tile", [(i, i ^ distance) for i in range(count)])


def on_device(
    pixels,
    buckets,
    slot_owner_table,
    out_grad,
    master,
    left_stat,
    right_stat,
    left_root,
    right_root,
    vectors,
    moment,
):
    tile_count = lax.axis_size("tile")
    tile_place = lax.axis_index("tile")
    slot_count = pixels.shape[2]
    group_count = tile_count // STRIPS
    pairs = group_count // 2
    owned = master.shape[0]
    slots = owned * tile_count
    batch_count = lax.axis_size("batch")
    spot = lax.axis_index("batch").astype(jnp.int32).reshape(1)
    extra = extra_of(owned, batch_count)
    strips = share_out(pixels.reshape((tile_count,) + pixels.shape[3:]), "tile")
    dense = pack(master)
    paired = tile_count <= 8
    if paired:
        mine = [dense] + [swap(dense, 2 * k) for k in range(1, tile_count // 2)]
        pieces = mine + [swap(piece, 1) for piece in mine]
    else:
        pieces = [lax.all_gather(dense, "tile", axis=0, tiled=True)]

    numbers = jnp.arange(slots, dtype=jnp.int32)
    slot_of = jnp.sum(
        jnp.where(slot_owner_table[None, :] == numbers[:, None], numbers[None, :], 0), axis=1
    )
    owner = slot_of // owned
    within = slot_of - owner * owned
    place_of = within + (owned + extra) * owner
    if paired:
        apart = owner ^ tile_place
        apart = (apart & 1) * (tile_count // 2) + (apart >> 1)
        slot_of = within + owned * apart
        place_of = within + (owned + extra) * apart
    image_ids = lax.dynamic_index_in_dim(
        buckets.reshape(group_count, slot_count), tile_place, 1, keepdims=False
    )
    turned = image_ids >= 2
    heights = jnp.where(image_ids == 0, 5 * CH // 9, jnp.where(image_ids == 1, 7 * CH // 9, CH))
    breadths = jnp.where(image_ids == 0, CW, jnp.where(image_ids == 1, 7 * CW // 9, 5 * CW // 9))
    sizes = jnp.stack(
        [
            jnp.where(turned, breadths, heights),
            jnp.where(turned, heights, breadths),
            turned,
        ],
        axis=1,
    )
    sizes = sizes.reshape(-1).astype(jnp.int32)

    two = 6 * C2 + HID2 + C2
    vec_two = jnp.concatenate([vectors[: 6 * C2], vectors[6 * C2 + HID2 : two]]).reshape(7, C2)
    vec_hid_two = vectors[6 * C2 : 6 * C2 + HID2].reshape(1, HID2)
    wide_end = two + 7 * C3
    vec_three = jnp.concatenate([vectors[two:wide_end], vectors[wide_end + HID3 :]])
    vec_three = jnp.pad(vec_three.reshape(8, C3), ((0, 0), (0, WIDE - C3)))
    vec_hid_three = vectors[wide_end : wide_end + HID3].reshape(1, HID3)

    flips = turned.reshape(-1, 1, 1, 1)
    goal = out_grad.reshape(2 * pairs, H3, W3, C3)
    goal = jnp.where(flips, goal.transpose(0, 2, 1, 3), goal)[:, :LINES]
    goal = goal.reshape(pairs, 2, LINES, W3, C3).transpose(0, 2, 3, 1, 4)
    goal = goal.reshape(pairs, LINES, 2 * W3, C3)
    goal = jnp.pad(goal, ((0, 0), (0, 0), (0, LINE - 2 * W3), (0, WIDE - C3)))
    goal = goal.reshape(pairs, AREA, WIDE)

    result, pixel_back, near, far = run_main(
        slot_of,
        place_of,
        sizes,
        strips,
        goal,
        (vec_two, vec_hid_two, vec_three, vec_hid_three),
        pieces,
        extra,
    )
    result = result.reshape(pairs, LINES, LINE, WIDE)[:, :, : 2 * W3, :C3]
    result = result.reshape(pairs, LINES, W3, 2, C3).transpose(0, 3, 1, 2, 4)
    result = result.reshape(2 * pairs, LINES, W3, C3)
    result = jnp.pad(result, ((0, 0), (0, H3 - LINES), (0, 0), (0, 0)))
    result = jnp.where(flips, result.transpose(0, 2, 1, 3), result)

    near = near.reshape(-1, owned + extra, HALF, 128)
    far = far.reshape(near.shape)
    returned = share_out(pixel_back, "tile").astype(f32).reshape(pixels.shape)
    result = result.reshape(out_grad.shape)
    if paired:
        own, *parts = fold_pair(near, swap(far, 1))
        pieces = [own] + [swap(part, 2 * k + 2) for k, part in enumerate(parts)]
    else:
        pieces = list(share_out(jnp.concatenate([near, far], axis=0), "tile"))
    result, returned, pieces = lax.optimization_barrier((result, returned, pieces))
    own, *parts = fold_tile(spot, pieces, batch_count)
    parts = [
        lax.ppermute(part, "batch", [(i, (i + k + 1) % batch_count) for i in range(batch_count)])
        for k, part in enumerate(parts)
    ]
    quarter, norm = fold_batch(spot, [own] + parts, owned, tile_count)
    quarters = [quarter] + [
        lax.ppermute(quarter, "batch", [(i, (i + k) % batch_count) for i in range(batch_count)])
        for k in range(1, batch_count)
    ]
    norm = share_out(norm, ("batch", "tile"))
    block_grad, left_new, right_new, master_new, weight_copy, whole_vector, clip = update(
        spot, norm, quarters, extra, master, left_stat, right_stat, left_root, right_root
    )
    clip_norm = clip[0, 0]
    share = vectors.shape[0] // tile_count
    whole_vector = whole_vector.reshape(-1)
    vec_grad = lax.dynamic_slice_in_dim(whole_vector, tile_place * share, share, 0)
    vec_moment = moment + vec_grad * vec_grad
    own_vectors = lax.dynamic_slice_in_dim(vectors, tile_place * share, share, 0)
    vec_new = own_vectors - rate_vector * vec_grad / (jnp.sqrt(vec_moment) + eps_adagrad)
    return (
        result,
        returned,
        clip_norm,
        block_grad,
        left_new,
        right_new,
        master_new,
        weight_copy,
        vec_grad,
        vec_moment,
        vec_new,
    )


def solution(mesh):
    placed = (
        P("batch", "tile", None, None, None, None),
        P("batch"),
        P(),
        P("batch", "tile", None, None, None, None, None),
        P("tile", None, None),
        P("tile", None, None),
        P("tile", None, None),
        P("tile", None, None),
        P("tile", None, None),
        P(),
        P("tile"),
    )
    return jax.shard_map(
        on_device,
        mesh=mesh,
        in_specs=placed,
        out_specs=(
            P("batch", "tile", None, None, None, None, None),
            P("batch", "tile", None, None, None, None),
            P(),
            P("tile", None, None),
            P("tile", None, None),
            P("tile", None, None),
            P("tile", None, None),
            P("tile", None, None),
            P("tile"),
            P("tile"),
            P("tile"),
        ),
        check_vma=False,
    )
```

```python
import functools

import jax
import jax.numpy as jnp
from jax import lax
from jax.experimental import pallas as pl
from jax.experimental.pallas import tpu as pltpu
from jax.sharding import PartitionSpec as P

C2 = 128
HID2 = 512
C3 = 320
HID3 = 1280
CH = 36
CW = 36
STRIPS = 4
BS = 64
SR = CH // STRIPS
H3 = CH // 2
W3 = CW // 2
LONG = 7 * CH // 9
LINES = LONG // 2
WIDE = 384
LINE = 40
AREA = LINES * LINE
STEP = 2 * LINE
STEPS = AREA // STEP
HALF = BS // 2

eps_norm = 1e-05
clip_limit = 1.0
rate_matrix = 0.3
rate_vector = 0.3
eps_adagrad = 1e-08
f32 = jnp.float32
bf16 = jnp.bfloat16

SHAPES = [(C2, HID2), (HID2, C2), (9 * C2, C3), (C3, HID3), (HID3, C3)]
USED = sum(rows // BS * (cols // BS) for rows, cols in SHAPES)
VEC_ROWS = (6 * C2 + HID2 + C2 + C3 + 6 * C3 + HID3 + C3) // 128


def extra_of(owned, groups):
    extra = -(-VEC_ROWS // HALF)
    return extra + -(owned + extra) % groups


def product(left, right):
    return jnp.dot(left, right, preferred_element_type=f32)


def product_nt(left, right):
    return lax.dot_general(left, right, (((1,), (1,)), ((), ())), preferred_element_type=f32)


def product_tn(left, right):
    return lax.dot_general(left, right, (((0,), (0,)), ((), ())), preferred_element_type=f32)


def gelu_pair(values):
    bell = jnp.exp2(values * values * (-0.5 * 1.4426950408889634))
    step = pl.reciprocal(1.0 + (0.3275911 * 0.7071067811865476) * jnp.abs(values), approx=True)
    tail = step * (
        0.5 * 0.254829592
        + step
        * (
            0.5 * -0.284496736
            + step
            * (0.5 * 1.421413741 + step * (0.5 * -1.453152027 + step * (0.5 * 1.061405429)))
        )
    )
    tail = tail * bell
    share = jnp.where(values >= 0.0, 1.0 - tail, tail)
    return (values * share, share + values * (bell * 0.3989422804014327))


def fold(values):
    chans = values.shape[-1]
    return jnp.sum(values.reshape(-1, 8, chans), axis=0)


def by_image(total):
    total = total + pltpu.roll(total, 4, 0)
    total = total + pltpu.roll(total, 2, 0)
    return jnp.sum(total, axis=1, keepdims=True)


def line(pattern):
    return jnp.concatenate([pattern] * (LINE // 8), axis=0)


def spread(pattern, chans):
    return jnp.broadcast_to(pattern, (8, chans))


def affine(values, factor, shift):
    tiles = values.reshape(-1, 8, values.shape[-1])
    return (tiles * factor + shift).reshape(values.shape)


def scaled(values, factor):
    tiles = values.reshape(-1, 8, values.shape[-1])
    return (tiles * factor).reshape(values.shape)


def from_left(values):
    return pltpu.roll(values, 2, 0)


def from_right(values):
    return pltpu.roll(values, values.shape[0] - 2, 0)


def rounded(values):
    return values.astype(bf16).astype(f32)


def widen(values):
    return jnp.concatenate([values] * (WIDE // 128), axis=-1)


def norm_terms(total, square, count):
    mean = by_image(total) / count
    scaling = lax.rsqrt(by_image(square) / count - mean * mean + eps_norm)
    return (mean, scaling)


def sweep(visit, start):
    return lax.fori_loop(0, STEPS, visit, start, unroll=True)


def step_rows(k, lines=0):
    start = k * STEP + lines * LINE
    return pl.ds(start if isinstance(k, int) else pl.multiple_of(start, LINE), STEP)


def held_in(space, *arrays):
    return [pltpu.with_memory_space_constraint(array, space) for array in arrays]


VMEM_BLOCK = pl.BlockSpec(memory_space=pltpu.VMEM)
HBM = pl.BlockSpec(memory_space=pltpu.HBM)
SMEM = pl.BlockSpec(memory_space=pltpu.SMEM)
ROOMY = pltpu.CompilerParams(vmem_limit_bytes=40 * 1024 * 1024)


class Geometry:
    def __init__(self, size_ref, pair):
        parity = lax.broadcasted_iota(jnp.int32, (8, 128), 0) % 2
        high, broad, turned = (
            jnp.where(parity == 0, size_ref[pair * 6 + n], size_ref[pair * 6 + 3 + n])
            for n in range(3)
        )
        self.high = high
        self.count_two = (high * broad * C2).astype(f32)[:, :1]
        self.high3 = (high + 1) // 2
        broad3 = (broad + 1) // 2
        self.count_three = (self.high3 * broad3 * C3).astype(f32)[:, :1]
        place = lax.broadcasted_iota(jnp.int32, (LINE, 128), 0) // 2
        inside = lax.broadcasted_iota(jnp.int32, (LINE, 128), 0) < 2 * W3
        self.reach = []
        self.col_share = []
        for pc in range(2):
            column = 2 * place + pc
            self.reach.append(jnp.where(inside & (column < line(broad)), line(high), 0))
            edge = (column == 0) | (column == line(broad) - 1)
            self.col_share.append(jnp.where(edge, 0.5, 1.0 / 3.0))
        self.reach3 = jnp.where(inside & (place < line(broad3)), line(self.high3), 0)
        edge3 = (place == 0) | (place == line(broad3) - 1)
        self.col_share3 = jnp.where(edge3, 0.5, 1.0 / 3.0)
        self.flipped = jnp.concatenate([turned] * (STEP // 8), axis=0) > 0

    def share(self, plane, k):
        pr, pc = plane // 2, plane % 2
        return self.lines(4 * k + pr, 2, self.reach[pc], self.col_share[pc], self.high)

    def share3(self, k):
        return self.lines(2 * k, 1, self.reach3, self.col_share3, self.high3)

    def lines(self, row, stride, reach, col_share, height):
        parts = []
        for n in range(2):
            here = row + stride * n
            row_share = jnp.where((here == 0) | (here == height - 1), 0.5, 1.0 / 3.0)
            parts.append(jnp.where(here < reach, line(row_share) * col_share, 0.0))
        return jnp.concatenate(parts, axis=0)


def strip_place(pair, spot, strip_count):
    return lax.rem(pair * 8 + strip_count - 2 + spot, strip_count)


def each_image(size_ref, pair, visit):
    for image in range(2):
        way = size_ref[pair * 6 + 3 * image + 2]
        for flat in (True, False):

            @pl.when(way == (0 if flat else 1))
            def _():
                def one(r, carry):
                    for pr in range(2):
                        for pc in range(2):
                            line_place = pl.ds(r * LINE + image, W3, stride=2)
                            if flat:
                                there = pl.ds((2 * r + pr) * LINE + pc, W3, stride=2)
                            else:
                                there = pl.ds(pc * LINE + 2 * r + pr, W3, stride=2 * LINE)
                            visit(image, pr * 2 + pc, line_place, there)
                    return carry

                lax.fori_loop(0, LINES, one, 0)


def row_windows(col_ref, pc, k):
    both = col_ref[pc, step_rows(k, 1)] + col_ref[2 + pc, step_rows(k, 1)]
    return (both + col_ref[2 + pc, step_rows(k)], both + col_ref[pc, step_rows(k, 2)])


def put_col_windows(col_ref, pr, k, even, odd):
    both = even + odd
    col_ref[pr * 2, step_rows(k, 1)] = both + from_left(odd)
    col_ref[pr * 2 + 1, step_rows(k, 1)] = both + from_right(even)


def clear_edges(col_ref):
    zero_line = jnp.zeros((LINE, C2), f32)
    for plane in range(4):
        col_ref[plane, 0:LINE] = zero_line
        col_ref[plane, AREA + LINE : AREA + 2 * LINE] = zero_line


def entry_kernel(
    pairs,
    strip_count,
    size_ref,
    strips_ref,
    vec_two_ref,
    x_out,
    inv_out,
    pool_out,
    mix_out,
    stat_out,
    image_ref,
    col_ref,
):
    pair = pl.program_id(0) if pairs > 1 else 0
    x_ref, inv_ref, pool_ref, mix_ref = (ref.at[0] for ref in (x_out, inv_out, pool_out, mix_out))
    shape = Geometry(size_ref, pair)
    gain1, bias1, scale1 = (vec_two_ref[n : n + 1] for n in range(3))
    clear_edges(col_ref)

    def to_rows(within, carry):
        for spot in range(2 * STRIPS):
            image, strip = spot // STRIPS, spot % STRIPS
            start = pl.multiple_of((strip * SR + within) * LINE, LINE)
            source = strip_place(pair, spot, strip_count)
            image_ref[image, pl.ds(start, CW)] = strips_ref[source, within].astype(f32)
        return carry

    lax.fori_loop(0, SR, to_rows, 0)

    def take_in(image, plane, line_place, there):
        x_ref[plane, line_place] = image_ref[image, there]

    each_image(size_ref, pair, take_in)

    def arrange(k, carry):
        total, square = carry
        rows = step_rows(k)
        for plane in range(4):
            share = shape.share(plane, k)
            inv_ref[plane, rows] = share
            values = jnp.where(share > 0.0, x_ref[plane, rows], 0.0)
            x_ref[plane, rows] = values
            total = total + fold(values)
            square = square + fold(values * values)
        return (total, square)

    nothing = jnp.zeros((8, C2), f32)
    total, square = sweep(arrange, (nothing, nothing))
    mean1, scaling1 = norm_terms(total, square, shape.count_two)
    factor1 = scaling1 * gain1
    shift1 = bias1 - mean1 * scaling1 * gain1

    def window_cols(k, carry):
        rows = step_rows(k)
        for pr in range(2):
            masked = []
            for pc in range(2):
                plane = pr * 2 + pc
                normal = rounded(affine(x_ref[plane, rows], factor1, shift1))
                masked.append(jnp.where(inv_ref[plane, rows] > 0.0, normal, 0.0))
            put_col_windows(col_ref, pr, k, *masked)
        return carry

    sweep(window_cols, 0)

    def mix(k, carry):
        total, square = carry
        rows = step_rows(k)
        for pc in range(2):
            windows = row_windows(col_ref, pc, k)
            for pr in range(2):
                plane = pr * 2 + pc
                values = x_ref[plane, rows]
                share = inv_ref[plane, rows]
                pooled = windows[pr] * share - rounded(affine(values, factor1, shift1))
                pooled = jnp.where(share > 0.0, pooled, 0.0)
                mixed = values + scale1 * pooled
                pool_ref[plane, rows] = pooled
                mix_ref[plane, rows] = mixed
                total = total + fold(mixed)
                square = square + fold(mixed * mixed)
        return (total, square)

    total, square = sweep(mix, (nothing, nothing))
    mean2, scaling2 = norm_terms(total, square, shape.count_two)
    for n, value in enumerate((mean1, scaling1, mean2, scaling2)):
        stat_out[0, n] = spread(value, 128)


def pair_specs(pairs, shapes, mode=None):
    if pairs == 1:
        return [VMEM_BLOCK] * len(shapes)
    return [
        pl.BlockSpec(
            (1,) + shape, lambda t, rank=len(shape): (t,) + (0,) * rank, pipeline_mode=mode
        )
        for shape in shapes
    ]


def whole_specs(pairs, shapes):
    if pairs == 1:
        return [VMEM_BLOCK] * len(shapes)
    return [
        pl.BlockSpec(
            shape,
            lambda t, rank=len(shape): (0,) * rank,
            pipeline_mode=pl.Buffered(1),
        )
        for shape in shapes
    ]


def pair_arrays(pairs, shapes, kinds):
    make = pltpu.VMEM if pairs == 1 else jax.ShapeDtypeStruct
    return [make((pairs,) + shape, kind) for shape, kind in zip(shapes, kinds)]


STATE = [(4, AREA, C2)] * 4 + [(4, 8, 128)]


def run_entry(sizes, strips, vec_two):
    strip_count = strips.shape[0]
    pairs = strip_count // 8
    return pl.pallas_call(
        functools.partial(entry_kernel, pairs, strip_count),
        grid=() if pairs == 1 else (pairs,),
        in_specs=[SMEM] + whole_specs(pairs, [strips.shape, vec_two.shape]),
        out_specs=pair_specs(pairs, STATE),
        out_shape=pair_arrays(pairs, STATE, [f32] * 5),
        scratch_shapes=[
            pltpu.VMEM((2, CH * LINE, C2), f32),
            pltpu.VMEM((4, AREA + 2 * LINE, C2), f32),
        ],
        compiler_params=ROOMY,
        name="entry",
    )(sizes, strips, vec_two)


def main_kernel(pairs, strip_count, slots, extra, piece_count, *refs):
    fixed, refs = refs[:14], refs[14:]
    inner_kernel(pairs, strip_count, slots, extra, refs[:piece_count], *fixed, *refs[piece_count:])


def inner_kernel(
    pairs,
    strip_count,
    slots,
    extra,
    piece_refs,
    slot_ref,
    near_place,
    far_place,
    size_ref,
    x_in,
    inv_in,
    pool_in,
    mix_in,
    stat_in,
    goal_ref,
    vec_two_ref,
    vec_hid_two_ref,
    vec_three_ref,
    vec_hid_three_ref,
    result_ref,
    pixel_ref,
    near_ref,
    far_ref,
    gathered_ref,
    image_ref,
    col_ref,
    back_ref,
    zed_ref,
    dx_ref,
    hid_ref,
    u_ref,
    g_ref,
    h_ref,
    dy_ref,
    patch_ref,
    dpatch_ref,
    inv3_ref,
    e_ref,
    col3_ref,
    pool3_ref,
    mix3_ref,
    dx3_ref,
    hid3_ref,
    dhid3_ref,
    u3_ref,
    g3_ref,
    h3_ref,
    dy3_ref,
    dpre_ref,
    w1_ref,
    w2_ref,
    we_ref,
    w3_ref,
    w4_ref,
    gw1_ref,
    gw2_ref,
    gwe_ref,
    gw3_ref,
    gw4_ref,
    acc_two,
    acc_hid_two,
    acc_three,
    acc_hid_three,
    flat_ref,
):
    pair = pl.program_id(0) if pairs > 1 else 0
    weights = [w1_ref, w2_ref, we_ref, w3_ref, w4_ref]
    grads = [gw1_ref, gw2_ref, gwe_ref, gw3_ref, gw4_ref]
    x_ref, inv_ref, pool_ref, mix_ref, stat_ref = (
        ref.at[0] for ref in (x_in, inv_in, pool_in, mix_in, stat_in)
    )
    left_half = lax.broadcasted_iota(jnp.int32, (HALF, 128), 1) < BS

    def at_pair(number, act):
        if pairs == 1:
            act()
        else:
            pl.when(pair == number)(act)

    def begin():
        count = slots // len(piece_refs)
        for n, ref in enumerate(piece_refs):
            gathered_ref[n * count : n * count + count] = ref[...]
        acc_two[...] = jnp.zeros(acc_two.shape, f32)
        acc_hid_two[...] = jnp.zeros(acc_hid_two.shape, f32)
        acc_three[...] = jnp.zeros(acc_three.shape, f32)
        acc_hid_three[...] = jnp.zeros(acc_hid_three.shape, f32)
        offset = 0
        for (rows, cols), ref in zip(SHAPES, weights):
            wide = cols // BS
            for rb in range(rows // BS):
                for cb in range(0, wide, 2):
                    number = offset + rb * wide + cb
                    first = gathered_ref[slot_ref[number]]
                    turned = pltpu.roll(first, BS, 1)
                    if cb + 1 < wide:
                        second = gathered_ref[slot_ref[number + 1]]
                        top = jnp.where(left_half, first, pltpu.roll(second, BS, 1))
                        low = jnp.where(left_half, turned, second)
                    else:
                        top = jnp.where(left_half, first, 0.0)
                        low = jnp.where(left_half, turned, 0.0)
                    place = slice(cb * BS, cb * BS + 128)
                    ref[rb * BS : rb * BS + HALF, place] = top
                    ref[rb * BS + HALF : rb * BS + BS, place] = low
            offset += rows // BS * wide
        w3_ref[C3:, :] = jnp.zeros((WIDE - C3, HID3), bf16)

    at_pair(0, begin)
    shape = Geometry(size_ref, pair)
    count_two, count_three, flipped = shape.count_two, shape.count_three, shape.flipped
    nothing = jnp.zeros((8, C2), f32)
    nothing3 = jnp.zeros((8, WIDE), f32)
    gain1, bias1, scale1 = (vec_two_ref[n : n + 1] for n in range(3))
    gain2, bias2, scale2, out_bias = (vec_two_ref[n : n + 1] for n in range(3, 7))
    embed_bias, gain3, bias3, scale3 = (vec_three_ref[n : n + 1] for n in range(4))
    gain4, bias4, scale4, out_bias3 = (vec_three_ref[n : n + 1] for n in range(4, 8))
    mean1, scaling1, mean2, scaling2 = (stat_ref[n] for n in range(4))
    factor2 = scaling2 * gain2
    shift2 = bias2 - mean2 * scaling2 * gain2
    clear_edges(col_ref)
    for plane in range(4):
        zed_ref[plane, 0:LINE] = jnp.zeros((LINE, C2), f32)
    col3_ref[0:LINE] = jnp.zeros((LINE, WIDE), f32)
    col3_ref[AREA + LINE : AREA + 2 * LINE] = jnp.zeros((LINE, WIDE), f32)

    def plane_rows(plane):
        return pl.ds(pl.multiple_of(plane * AREA, AREA), AREA)

    def branch(plane, carry):
        mixed = mix_ref[plane]
        low = affine(mixed, factor2, shift2).astype(bf16)
        h_ref[plane_rows(plane)] = low
        hid_ref[...] = product(low, w1_ref[...])

        def activate(k, carry):
            rows = step_rows(k)
            flat = pl.ds(pl.multiple_of(plane * AREA + k * STEP, STEP), STEP)
            for at in range(0, HID2, 128):
                lanes = slice(at, at + 128)
                active, slope = gelu_pair(hid_ref[rows, lanes] + vec_hid_two_ref[:, lanes])
                u_ref[flat, lanes] = active.astype(bf16)
                g_ref[flat, lanes] = slope.astype(bf16)
            return carry

        sweep(activate, 0)
        out = product(u_ref[plane_rows(plane)], w2_ref[...]) + out_bias
        zed = jnp.where(inv_ref[plane] > 0.0, mixed + scale2 * out, 0.0)
        zed_ref[plane, LINE : LINE + AREA] = rounded(zed)
        return carry

    lax.fori_loop(0, 4, branch, 0)

    def patches(k, carry):
        rows = step_rows(k)
        taps = []
        for ky in range(3):
            pr = (0 if ky == 1 else 1) * 2
            source = step_rows(k, 0 if ky == 0 else 1)
            even = zed_ref[pr, source]
            odd = zed_ref[pr + 1, source]
            taps.append((from_left(odd), even, odd))
        for ky in range(3):
            for kx in range(3):
                at = (3 * ky + kx) * C2
                tap = taps[ky][kx]
                if ky != kx:
                    tap = jnp.where(flipped, taps[kx][ky], tap)
                patch_ref[rows, at : at + C2] = tap.astype(bf16)
        return carry

    sweep(patches, 0)
    e_ref[...] = product(patch_ref[...], we_ref[...])

    def embed(k, carry):
        total, square = carry
        rows = step_rows(k)
        share = shape.share3(k)
        inv3_ref[rows] = share
        out = jnp.where(widen(share) > 0.0, e_ref[rows] + embed_bias, 0.0)
        e_ref[rows] = out
        return (total + fold(out), square + fold(out * out))

    total, square = sweep(embed, (nothing3, nothing3))
    mean3, scaling3 = norm_terms(total, square, count_three)
    factor3 = scaling3 * gain3
    shift3 = bias3 - mean3 * scaling3 * gain3

    def window_cols3(k, carry):
        rows = step_rows(k)
        normal = rounded(affine(e_ref[rows], factor3, shift3))
        masked = jnp.where(widen(inv3_ref[rows]) > 0.0, normal, 0.0)
        col3_ref[step_rows(k, 1)] = masked + from_left(masked) + from_right(masked)
        return carry

    sweep(window_cols3, 0)

    def row_windows3(k):
        return col3_ref[step_rows(k)] + col3_ref[step_rows(k, 1)] + col3_ref[step_rows(k, 2)]

    def mix3(k, carry):
        total, square = carry
        rows = step_rows(k)
        values = e_ref[rows]
        share = widen(inv3_ref[rows])
        pooled = row_windows3(k) * share - rounded(affine(values, factor3, shift3))
        pooled = jnp.where(share > 0.0, pooled, 0.0)
        mixed = values + scale3 * pooled
        pool3_ref[rows] = pooled
        mix3_ref[rows] = mixed
        return (total + fold(mixed), square + fold(mixed * mixed))

    total, square = sweep(mix3, (nothing3, nothing3))
    mean4, scaling4 = norm_terms(total, square, count_three)
    factor4 = scaling4 * gain4
    shift4 = bias4 - mean4 * scaling4 * gain4
    normal4 = (spread(scaling4, WIDE), spread(-mean4 * scaling4, WIDE))

    def prepare3(k, d_bias):
        rows = step_rows(k)
        h3_ref[rows] = affine(mix3_ref[rows], factor4, shift4).astype(bf16)
        goal = goal_ref[0, rows].astype(f32)
        goal = jnp.where(widen(inv3_ref[rows]) > 0.0, goal, 0.0)
        low_goal = (scale4 * goal).astype(bf16)
        dy3_ref[rows] = low_goal
        return d_bias + fold(low_goal.astype(f32))

    acc_three[7] += sweep(prepare3, nothing3)
    hid3_ref[...] = product(h3_ref[...], w3_ref[...])
    dhid3_ref[...] = product_nt(dy3_ref[...], w4_ref[...])

    def activate3(k, sums):
        rows = step_rows(k)
        new = []
        for n, at in enumerate(range(0, HID3, 128)):
            lanes = slice(at, at + 128)
            active, slope = gelu_pair(hid3_ref[rows, lanes] + vec_hid_three_ref[:, lanes])
            u3_ref[rows, lanes] = active.astype(bf16)
            low = (slope * dhid3_ref[rows, lanes]).astype(bf16)
            g3_ref[rows, lanes] = low
            new.append(sums[n] + fold(low.astype(f32)))
        return tuple(new)

    sums = sweep(activate3, (nothing,) * (HID3 // 128))
    for n, value in enumerate(sums):
        acc_hid_three[:, n * 128 : n * 128 + 128] += value

    def keep(ref, value):
        if pairs == 1:
            ref[...] = value.astype(ref.dtype)
        else:

            @pl.when(pair == 0)
            def _():
                ref[...] = value

            @pl.when(pair > 0)
            def _():
                ref[...] += value

    result_ref[0] = product(u3_ref[...], w4_ref[...])
    dx3_ref[...] = product_nt(g3_ref[...], w3_ref[...])
    keep(gw3_ref, product_tn(h3_ref[...], g3_ref[...]))
    keep(gw4_ref, product_tn(u3_ref[...], dy3_ref[...]))

    def finish3(k, carry):
        d_scale, d_shift, d_gain = carry
        rows = step_rows(k)
        valid = widen(inv3_ref[rows]) > 0.0
        mixed = mix3_ref[rows]
        out = jnp.where(valid, result_ref[0, rows] + out_bias3, 0.0)
        result_ref[0, rows] = mixed + scale4 * out
        d_scale = d_scale + fold(out * goal_ref[0, rows].astype(f32))
        d_low = dx3_ref[rows]
        normal = affine(mixed, *normal4)
        return (d_scale, d_shift + fold(d_low), d_gain + fold(d_low * normal))

    d_scale, d_shift, d_gain = sweep(finish3, (nothing3, nothing3, nothing3))
    acc_three[6] += d_scale
    acc_three[5] += d_shift
    acc_three[4] += d_gain
    mean_shift = by_image(d_shift * gain4) / count_three
    mean_gain = by_image(d_gain * gain4) / count_three
    back_gain4 = scaling4 * gain4
    back_mean4 = spread(-scaling4 * mean_shift, WIDE)
    back_normal4 = spread(scaling4 * mean_gain, WIDE)

    def unmix3(k, d_scale):
        rows = step_rows(k)
        share = widen(inv3_ref[rows])
        valid = share > 0.0
        normal = affine(mix3_ref[rows], *normal4)
        back = affine(dx3_ref[rows], back_gain4, back_mean4) - scaled(normal, back_normal4)
        d_mixed = jnp.where(valid, back + goal_ref[0, rows].astype(f32), 0.0)
        dx3_ref[rows] = d_mixed
        d_scale = d_scale + fold(pool3_ref[rows] * d_mixed)
        weighted = scale3 * d_mixed * share
        col3_ref[step_rows(k, 1)] = weighted + from_left(weighted) + from_right(weighted)
        return d_scale

    acc_three[3] += sweep(unmix3, nothing3)
    normal3 = (spread(scaling3, WIDE), spread(-mean3 * scaling3, WIDE))

    def unpool3(k, carry):
        d_shift, d_gain = carry
        rows = step_rows(k)
        valid = widen(inv3_ref[rows]) > 0.0
        d_normal = jnp.where(valid, row_windows3(k) - scale3 * dx3_ref[rows], 0.0)
        pool3_ref[rows] = d_normal
        normal = affine(e_ref[rows], *normal3)
        return (d_shift + fold(d_normal), d_gain + fold(d_normal * normal))

    d_shift, d_gain = sweep(unpool3, (nothing3, nothing3))
    acc_three[2] += d_shift
    acc_three[1] += d_gain
    mean_shift = by_image(d_shift * gain3) / count_three
    mean_gain = by_image(d_gain * gain3) / count_three
    back_gain3 = scaling3 * gain3
    back_mean3 = spread(-scaling3 * mean_shift, WIDE)
    back_normal3 = spread(scaling3 * mean_gain, WIDE)

    def unnorm3(k, d_bias):
        rows = step_rows(k)
        valid = widen(inv3_ref[rows]) > 0.0
        normal = affine(e_ref[rows], *normal3)
        back = affine(pool3_ref[rows], back_gain3, back_mean3) - scaled(normal, back_normal3)
        low = jnp.where(valid, dx3_ref[rows] + back, 0.0).astype(bf16)
        dpre_ref[rows] = low
        return d_bias + fold(low.astype(f32))

    acc_three[0] += sweep(unnorm3, nothing3)
    keep(gwe_ref, product_tn(patch_ref[...], dpre_ref[...]))
    dpatch_ref[0:AREA] = product_nt(dpre_ref[...], we_ref[...])
    dpatch_ref[AREA : AREA + LINE] = jnp.zeros((LINE, 9 * C2), f32)

    def gather_back(k, carry):
        rows = step_rows(k)

        def tap(ky, kx, source):
            at = (3 * ky + kx) * C2
            value = dpatch_ref[source, at : at + C2]
            if ky != kx:
                at = (3 * kx + ky) * C2
                value = jnp.where(flipped, dpatch_ref[source, at : at + C2], value)
            return value

        sources = []
        for ky in range(3):
            source = step_rows(k, 1 if ky == 0 else 0)
            sources.append(
                (tap(ky, 1, source), tap(ky, 2, source) + from_right(tap(ky, 0, source)))
            )
        for pc in range(2):
            for pr, value in ((0, sources[1][pc]), (1, sources[2][pc] + sources[0][pc])):
                plane = pr * 2 + pc
                valid = inv_ref[plane, rows] > 0.0
                zed_ref[plane, rows] = jnp.where(valid, rounded(value), 0.0)
        return carry

    sweep(gather_back, 0)

    normal2 = (spread(scaling2, C2), spread(-mean2 * scaling2, C2))

    def unbranch(plane, carry):
        d_out_bias, d_shift, d_gain, sums = carry
        flat = plane_rows(plane)
        low_goal = (scale2 * zed_ref[plane, 0:AREA]).astype(bf16)
        dy_ref[flat] = low_goal
        hid_ref[...] = product_nt(low_goal, w2_ref[...])

        def slopes(k, sums):
            rows = step_rows(k)
            part = pl.ds(pl.multiple_of(plane * AREA + k * STEP, STEP), STEP)
            new = []
            for n, at in enumerate(range(0, HID2, 128)):
                lanes = slice(at, at + 128)
                low = (g_ref[part, lanes].astype(f32) * hid_ref[rows, lanes]).astype(bf16)
                g_ref[part, lanes] = low
                new.append(sums[n] + fold(low.astype(f32)))
            return tuple(new)

        sums = sweep(slopes, sums)
        d_low = product_nt(g_ref[flat], w1_ref[...])
        dx_ref[plane] = d_low
        normal = affine(mix_ref[plane], *normal2)
        return (
            d_out_bias + fold(low_goal.astype(f32)),
            d_shift + fold(d_low),
            d_gain + fold(d_low * normal),
            sums,
        )

    d_out_bias, d_shift, d_gain, sums = lax.fori_loop(
        0, 4, unbranch, (nothing, nothing, nothing, (nothing,) * (HID2 // 128))
    )
    for n, value in enumerate(sums):
        acc_hid_two[:, n * 128 : n * 128 + 128] += value
    acc_two[6] += d_out_bias
    acc_two[4] += d_shift
    acc_two[3] += d_gain
    mean_shift = by_image(d_shift * gain2) / count_two
    mean_gain = by_image(d_gain * gain2) / count_two
    keep(gw1_ref, product_tn(h_ref[...], g_ref[...]))
    new_gw2 = product_tn(dy_ref[...], u_ref[...]).T
    keep(gw2_ref, new_gw2)
    d_scale = fold(w2_ref[...].astype(f32) * new_gw2) + out_bias * d_out_bias
    acc_two[5] += d_scale / scale2

    back_gain2 = scaling2 * gain2
    back_mean2 = spread(-scaling2 * mean_shift, C2)
    back_normal2 = spread(scaling2 * mean_gain, C2)

    def unmix(k, d_scale):
        rows = step_rows(k)
        for pr in range(2):
            weighted = []
            for pc in range(2):
                plane = pr * 2 + pc
                share = inv_ref[plane, rows]
                normal = affine(mix_ref[plane, rows], *normal2)
                back = affine(dx_ref[plane, rows], back_gain2, back_mean2)
                back = back - scaled(normal, back_normal2)
                d_mixed = jnp.where(share > 0.0, zed_ref[plane, rows] + back, 0.0)
                dx_ref[plane, rows] = d_mixed
                d_scale = d_scale + fold(pool_ref[plane, rows] * d_mixed)
                weighted.append(scale1 * d_mixed * share)
            put_col_windows(col_ref, pr, k, *weighted)
        return d_scale

    acc_two[2] += sweep(unmix, nothing)
    normal1 = (spread(scaling1, C2), spread(-mean1 * scaling1, C2))

    def unpool(k, carry):
        d_shift, d_gain = carry
        rows = step_rows(k)
        for pc in range(2):
            windows = row_windows(col_ref, pc, k)
            for pr in range(2):
                plane = pr * 2 + pc
                valid = inv_ref[plane, rows] > 0.0
                d_normal = windows[pr] - scale1 * dx_ref[plane, rows]
                d_normal = jnp.where(valid, d_normal, 0.0)
                back_ref[plane, rows] = d_normal
                normal = affine(x_ref[plane, rows], *normal1)
                d_shift = d_shift + fold(d_normal)
                d_gain = d_gain + fold(d_normal * normal)
        return (d_shift, d_gain)

    d_shift, d_gain = sweep(unpool, (nothing, nothing))
    acc_two[1] += d_shift
    acc_two[0] += d_gain
    mean_shift = by_image(d_shift * gain1) / count_two
    mean_gain = by_image(d_gain * gain1) / count_two
    back_gain1 = scaling1 * gain1
    back_mean1 = spread(-scaling1 * mean_shift, C2)
    back_normal1 = spread(scaling1 * mean_gain, C2)

    def unnorm(k, carry):
        rows = step_rows(k)
        for plane in range(4):
            normal = affine(x_ref[plane, rows], *normal1)
            back = affine(back_ref[plane, rows], back_gain1, back_mean1)
            back = back - scaled(normal, back_normal1)
            valid = inv_ref[plane, rows] > 0.0
            dx_ref[plane, rows] = jnp.where(valid, dx_ref[plane, rows] + back, 0.0)
        return carry

    sweep(unnorm, 0)

    def give_back(image, plane, line_place, there):
        image_ref[image, there] = dx_ref[plane, line_place]

    image_ref[...] = jnp.zeros(image_ref.shape, f32)
    each_image(size_ref, pair, give_back)

    def from_rows(within, carry):
        for spot in range(2 * STRIPS):
            image, strip = spot // STRIPS, spot % STRIPS
            start = pl.multiple_of((strip * SR + within) * LINE, LINE)
            target = strip_place(pair, spot, strip_count)
            pixel_ref[target, within] = image_ref[image, pl.ds(start, CW)].astype(bf16)
        return carry

    lax.fori_loop(0, SR, from_rows, 0)
    def finish():
        def put_block(number, block):
            near_ref[near_place[number]] = block
            far_ref[far_place[number]] = block

        offset = 0
        for (rows, cols), ref in zip(SHAPES, grads):
            wide = cols // BS
            for rb in range(rows // BS):
                for cb in range(0, wide, 2):
                    number = offset + rb * wide + cb
                    at = slice(cb * BS, cb * BS + 128)
                    top = ref[rb * BS : rb * BS + HALF, at].astype(bf16)
                    low = ref[rb * BS + HALF : rb * BS + BS, at].astype(bf16)
                    put_block(number, jnp.where(left_half, top, pltpu.roll(low, BS, 1)))
                    if cb + 1 < wide:
                        put_block(number + 1, jnp.where(left_half, pltpu.roll(top, BS, 1), low))
            offset += rows // BS * wide

        def filler(number, carry):
            put_block(number, jnp.zeros((HALF, 128), bf16))
            return carry

        lax.fori_loop(USED, slots, filler, 0)

        flat_ref[...] = jnp.zeros(flat_ref.shape, f32)

        def put(at, total, length):
            if at % 128:
                room = jnp.zeros((8, 128), f32)
                if total.shape[1] < length + BS:
                    total = jnp.concatenate([total, room], axis=1)
                total = pltpu.roll(total, BS, 1)
            whole = jnp.sum(total, axis=0, keepdims=True)
            done = -(at % 128)
            row = at // 128
            lane = 0
            while done < length:
                first = max(0, -done)
                last = min(128, length - done)
                flat_ref[row : row + 1, first:last] = whole[:, lane + first : lane + last]
                done += 128
                lane += 128
                row += 1

        at = 0
        for n in range(6):
            put(at, acc_two[n], C2)
            at += C2
        put(at, acc_hid_two[...], HID2)
        at += HID2
        put(at, acc_two[6], C2)
        at += C2
        for n in range(7):
            put(at, acc_three[n], C3)
            at += C3
        put(at, acc_hid_three[...], HID3)
        at += HID3
        put(at, acc_three[7], C3)
        packed = flat_ref[...].astype(bf16)
        stride = slots // strip_count + extra
        for n in range(extra):
            piece = packed[n * HALF : (n + 1) * HALF]

            def leave(target, carry):
                near_ref[target * stride + stride - extra + n] = piece
                far_ref[target * stride + stride - extra + n] = piece
                return carry

            lax.fori_loop(0, strip_count // 2, leave, 0)

    at_pair(pairs - 1, finish)


def run_main(places, sizes, state, goal, vectors, pieces, strips, extra):
    strip_count = strips.shape[0]
    pairs = goal.shape[0]
    slots = sum(piece.shape[0] for piece in pieces)
    half = (slots + extra * strip_count) // 2 + 1
    if pairs == 1:
        pieces = held_in(pltpu.VMEM, *pieces)
        state = held_in(pltpu.VMEM, *state)
    grad_kind = bf16 if pairs == 1 else f32
    plane_f32 = pltpu.VMEM((4, AREA, C2), f32)
    wide_f32 = pltpu.VMEM((AREA, WIDE), f32)
    wide_bf16 = pltpu.VMEM((AREA, WIDE), bf16)
    scratch = [
        pltpu.VMEM((slots, HALF, 128), bf16),
        pltpu.VMEM((2, CH * LINE, C2), f32),
        pltpu.VMEM((4, AREA + 2 * LINE, C2), f32),
        plane_f32,
        pltpu.VMEM((4, AREA + LINE, C2), f32),
        plane_f32,
        pltpu.VMEM((AREA, HID2), f32),
        pltpu.VMEM((4 * AREA, HID2), bf16),
        pltpu.VMEM((4 * AREA, HID2), bf16),
        pltpu.VMEM((4 * AREA, C2), bf16),
        pltpu.VMEM((4 * AREA, C2), bf16),
        pltpu.VMEM((AREA, 9 * C2), bf16),
        pltpu.VMEM((AREA + LINE, 9 * C2), f32),
        pltpu.VMEM((AREA, 128), f32),
        wide_f32,
        pltpu.VMEM((AREA + 2 * LINE, WIDE), f32),
        wide_f32,
        wide_f32,
        wide_f32,
        pltpu.VMEM((AREA, HID3), f32),
        pltpu.VMEM((AREA, HID3), f32),
        pltpu.VMEM((AREA, HID3), bf16),
        pltpu.VMEM((AREA, HID3), bf16),
        wide_bf16,
        wide_bf16,
        wide_bf16,
        pltpu.VMEM((C2, HID2), bf16),
        pltpu.VMEM((HID2, C2), bf16),
        pltpu.VMEM((9 * C2, WIDE), bf16),
        pltpu.VMEM((WIDE, HID3), bf16),
        pltpu.VMEM((HID3, WIDE), bf16),
        pltpu.VMEM((C2, HID2), grad_kind),
        pltpu.VMEM((HID2, C2), grad_kind),
        pltpu.VMEM((9 * C2, WIDE), grad_kind),
        pltpu.VMEM((WIDE, HID3), grad_kind),
        pltpu.VMEM((HID3, WIDE), grad_kind),
        pltpu.VMEM((7, 8, C2), f32),
        pltpu.VMEM((8, HID2), f32),
        pltpu.VMEM((8, 8, WIDE), f32),
        pltpu.VMEM((8, HID3), f32),
        pltpu.VMEM((extra * HALF, 128), f32),
    ]
    out_shapes = [strips.shape, (half, HALF, 128), (half, HALF, 128)]
    make = pltpu.VMEM if pairs == 1 else jax.ShapeDtypeStruct
    return pl.pallas_call(
        functools.partial(main_kernel, pairs, strip_count, slots, extra, len(pieces)),
        grid=() if pairs == 1 else (pairs,),
        in_specs=[SMEM] * 4
        + pair_specs(pairs, STATE + [goal.shape[1:]], pl.Buffered(1))
        + whole_specs(pairs, [array.shape for array in (*vectors, *pieces)]),
        out_specs=pair_specs(pairs, [(AREA, WIDE)]) + whole_specs(pairs, out_shapes),
        out_shape=pair_arrays(pairs, [(AREA, WIDE)], [f32])
        + [make(shape, bf16) for shape in out_shapes],
        scratch_shapes=scratch,
        compiler_params=pltpu.CompilerParams(
            vmem_limit_bytes=(46 if pairs == 1 else 60) * 1024 * 1024,
            fuse_transposed_lhs_in_matmul=True,
        ),
        name="blocks",
    )(*places, sizes, *state, goal, *vectors, *pieces)


def pack_kernel(master_ref, dense_ref):
    values = master_ref[...]
    dense_ref[...] = jnp.concatenate([values[:, :HALF], values[:, HALF:]], axis=2).astype(bf16)


def pack(master):
    owned = master.shape[0]
    return pl.pallas_call(
        pack_kernel,
        out_shape=jax.ShapeDtypeStruct((owned, HALF, 2 * BS), bf16),
        name="pack",
    )(master)


def fold_pair_kernel(near_ref, got_ref, own_ref, *part_refs):
    share = own_ref.shape[0]

    def one(n, carry):
        for k in range(len(part_refs) + 1):
            total = near_ref[k * share + n].astype(f32) + got_ref[k * share + n].astype(f32)
            if k == 0:
                own_ref[n] = total
            else:
                part_refs[k - 1][n] = total.astype(bf16)
        return carry

    lax.fori_loop(0, share, one, 0, unroll=4)


def fold_pair(near, got, groups):
    shape = ((near.shape[0] - 1) // groups,) + near.shape[1:]
    return pl.pallas_call(
        fold_pair_kernel,
        in_specs=[VMEM_BLOCK] * 2,
        out_specs=[VMEM_BLOCK] * groups,
        out_shape=[pltpu.VMEM(shape, f32)] + [pltpu.VMEM(shape, bf16)] * (groups - 1),
        compiler_params=ROOMY,
        name="fold_pair",
    )(*held_in(pltpu.VMEM, near, got))


def fold_tile_kernel(pieces, spot_ref, *refs):
    piece_refs, out_refs = refs[:pieces], refs[pieces:]
    groups = len(out_refs)
    share = out_refs[0].shape[0]
    starts = [lax.rem(spot_ref[0] + k, groups) * share for k in range(groups)]

    def one(n, carry):
        for start, out_ref in zip(starts, out_refs):
            total = piece_refs[0][start + n].astype(f32)
            for ref in piece_refs[1:]:
                total = total + ref[start + n].astype(f32)
            out_ref[n] = total.astype(out_ref.dtype)
        return carry

    lax.fori_loop(0, share, one, 0, unroll=share <= 16)


def fold_tile(spot, pieces, groups):
    shape = (pieces[0].shape[0] // groups,) + pieces[0].shape[1:]
    return pl.pallas_call(
        functools.partial(fold_tile_kernel, len(pieces)),
        in_specs=[SMEM] + [VMEM_BLOCK] * len(pieces),
        out_specs=[VMEM_BLOCK] * groups,
        out_shape=[pltpu.VMEM(shape, f32)] + [pltpu.VMEM(shape, bf16)] * (groups - 1),
        compiler_params=ROOMY,
        name="fold_tile",
    )(spot, *held_in(pltpu.VMEM, *pieces))


def fold_batch_kernel(owned, vector_weight, spot_ref, *refs):
    part_refs, (total_ref, norm_ref) = refs[:-2], refs[-2:]
    share = total_ref.shape[0]
    square = jnp.zeros((8, 128), f32)
    for n in range(share):
        total = part_refs[0][n].astype(f32)
        for ref in part_refs[1:]:
            total = total + ref[n].astype(f32)
        total_ref[n] = total.astype(bf16)
        weight = jnp.where(spot_ref[0] * share + n < owned, 1.0, vector_weight)
        square = square + weight * fold(total * total)
    square = jnp.sum(jnp.sum(square, axis=1, keepdims=True), axis=0, keepdims=True)
    norm_ref[...] = jnp.broadcast_to(square[None], norm_ref.shape)


def fold_batch(spot, parts, owned, tile_count):
    count = tile_count * len(parts)
    return pl.pallas_call(
        functools.partial(fold_batch_kernel, owned, 1.0 / tile_count),
        in_specs=[SMEM] + [VMEM_BLOCK] * len(parts),
        out_specs=[VMEM_BLOCK] * 2,
        out_shape=[pltpu.VMEM(parts[0].shape, bf16), pltpu.VMEM((count, 1, 128), f32)],
        name="fold_batch",
    )(spot, *held_in(pltpu.VMEM, *parts))


def update_kernel(owned, groups, spot_ref, norm_ref, *refs):
    quarters, refs = refs[:groups], refs[groups:]
    stat_hbm, out_hbm, (vector_ref, clip_ref), refs = refs[:5], refs[5:10], refs[10:12], refs[12:]
    stat_refs, out_refs, (in_sem, out_sem) = refs[:5], refs[5:10], refs[10:]
    master_ref, left_stat_ref, right_stat_ref, left_root_ref, right_root_ref = stat_refs
    grad_ref, left_ref, right_ref, new_ref, copy_ref = out_refs
    share = quarters[0].shape[0]
    spans = [(first, min(8, owned - first)) for first in range(0, owned, 8)]

    def copies_of(sources, targets, sems):
        return [
            [
                pltpu.make_async_copy(
                    source.at[pl.ds(*span)], target.at[pl.ds(*span)], sems.at[5 * n + k]
                )
                for k, (source, target) in enumerate(zip(sources, targets))
            ]
            for n, span in enumerate(spans)
        ]

    copies_in = copies_of(stat_hbm, stat_refs, in_sem)
    copies_out = copies_of(out_refs, out_hbm, out_sem)
    for copies in copies_in:
        for copy in copies:
            copy.start()
    norm = jnp.sqrt(jnp.sum(norm_ref[...], axis=0))
    factor = jnp.minimum(1.0, clip_limit / norm)
    left_half = lax.broadcasted_iota(jnp.int32, (HALF, 128), 1) < BS

    def summed(number):
        source = number // share
        local = number - source * share
        turn = lax.rem(spot_ref[0] - source + groups, groups)
        value = quarters[0][local].astype(f32)
        for k in range(1, groups):
            value = jnp.where(turn == k, quarters[k][local].astype(f32), value)
        return value * factor

    def one_group(first, count):
        sides = []
        for n in range(first, first + count, 2):
            dense = summed(n)
            turned = pltpu.roll(dense, BS, 1)
            if n + 1 < first + count:
                second = summed(n + 1)
                top = jnp.where(left_half, dense, pltpu.roll(second, BS, 1))
                low = jnp.where(left_half, turned, second)
                side = jnp.concatenate([top, low], axis=0)
                grad_ref[n + 1] = pltpu.roll(side, BS, 1)[:, :BS]
            else:
                side = jnp.concatenate([dense, turned], axis=0)[:, :BS]
            grad_ref[n] = side[:, :BS]
            sides.append(side.astype(bf16))
        wide = jnp.concatenate(sides, axis=1)
        order = count * BS
        row_block = lax.broadcasted_iota(jnp.int32, (order, order), 0) // BS
        col_block = lax.broadcasted_iota(jnp.int32, (order, order), 1) // BS
        diagonal = row_block == col_block
        here = pl.ds(first, count)
        tall = jnp.where(diagonal, jnp.concatenate([wide] * count, axis=0), 0.0)
        left = product_nt(tall, wide).reshape(count, BS, BS)
        left_ref[here] = 0.5 * left_stat_ref[here] + 0.5 * left
        right = product_tn(wide, wide)
        for n in range(count):
            at = n // 2 * 128
            block = right[n * BS : n * BS + BS, at : min(at + 128, order)]
            if n % 2:
                block = pltpu.roll(block, BS, 1)
            right_ref[first + n] = 0.5 * right_stat_ref[first + n] + 0.5 * block[:, :BS]
        roots = left_root_ref[here].reshape(order, BS).astype(bf16)
        stepped = jnp.where(diagonal, product(roots, wide), 0.0).astype(bf16)
        roots = right_root_ref[here].reshape(order, BS).astype(bf16)
        stepped = product(stepped, roots).reshape(count, BS, BS)
        new = master_ref[here] - rate_matrix * stepped
        new_ref[here] = new
        copy_ref[here] = new.astype(bf16)

    clip_ref[...] = norm
    for n in range(vector_ref.shape[0]):
        vector_ref[n] = summed(owned + n)
    for (first, count), arriving, leaving in zip(spans, copies_in, copies_out):
        for copy in arriving:
            copy.wait()
        for start in range(first, first + count, 4):
            one_group(start, min(4, first + count - start))
        for copy in leaving:
            copy.start()
    for leaving in copies_out:
        for copy in leaving:
            copy.wait()


def update(spot, norm, quarters, extra, *stats):
    shape = stats[0].shape
    groups = len(quarters)
    types = [f32] * 4 + [bf16]
    steps = -(-shape[0] // 8)
    return pl.pallas_call(
        functools.partial(update_kernel, shape[0], groups),
        in_specs=[SMEM] + [VMEM_BLOCK] * (groups + 1) + [HBM] * 5,
        out_specs=[HBM] * 5 + [VMEM_BLOCK] * 2,
        out_shape=[pltpu.HBM(shape, kind) for kind in types]
        + [
            jax.ShapeDtypeStruct((extra, HALF, 128), f32),
            jax.ShapeDtypeStruct((1, 128), f32),
        ],
        scratch_shapes=[pltpu.VMEM(shape, f32)] * 5
        + [pltpu.VMEM(shape, kind) for kind in types]
        + [
            pltpu.SemaphoreType.DMA((5 * steps,)),
            pltpu.SemaphoreType.DMA((5 * steps,)),
        ],
        compiler_params=ROOMY,
        name="update",
    )(spot, *held_in(pltpu.VMEM, norm, *quarters), *held_in(pltpu.HBM, *stats))


def share_out(pieces, axis):
    return lax.all_to_all(pieces, axis, split_axis=0, concat_axis=0, tiled=True)


def swap(piece, distance):
    count = lax.axis_size("tile")
    return lax.ppermute(piece, "tile", [(i, i ^ distance) for i in range(count)])


def on_device(
    pixels,
    buckets,
    slot_owner_table,
    out_grad,
    master,
    left_stat,
    right_stat,
    left_root,
    right_root,
    vectors,
    moment,
):
    tile_count = lax.axis_size("tile")
    tile_place = lax.axis_index("tile")
    slot_count = pixels.shape[2]
    group_count = tile_count // STRIPS
    pairs = group_count // 2
    owned = master.shape[0]
    slots = owned * tile_count
    batch_count = lax.axis_size("batch")
    spot = lax.axis_index("batch").astype(jnp.int32).reshape(1)
    extra = extra_of(owned, batch_count)
    strips = pixels.reshape((tile_count,) + pixels.shape[3:])
    strips, master = lax.optimization_barrier((strips, master))
    strips = share_out(strips, "tile")
    dense = pack(master)
    paired = tile_count <= 8
    if paired:
        mine = [dense] + [swap(dense, 2 * k) for k in range(1, tile_count // 2)]
        pieces = mine + [swap(piece, 1) for piece in mine]
    else:
        pieces = [lax.all_gather(dense, "tile", axis=0, tiled=True)]

    numbers = jnp.arange(slots, dtype=jnp.int32)
    slot_of = jnp.sum(
        jnp.where(slot_owner_table[None, :] == numbers[:, None], numbers[None, :], 0), axis=1
    )
    owner = slot_of // owned
    within = slot_of - owner * owned
    place_of = within + (owned + extra) * owner
    if paired:
        apart = owner ^ tile_place
        apart = (apart & 1) * (tile_count // 2) + (apart >> 1)
        slot_of = within + owned * apart
        place_of = within + (owned + extra) * apart
    half = (owned + extra) * tile_count // 2
    near_place = jnp.where(place_of < half, place_of, half)
    far_place = jnp.where(place_of < half, half, place_of - half)
    image_ids = lax.dynamic_index_in_dim(
        buckets.reshape(group_count, slot_count), tile_place, 1, keepdims=False
    )
    turned = image_ids >= 2
    heights = jnp.where(image_ids == 0, 5 * CH // 9, jnp.where(image_ids == 1, 7 * CH // 9, CH))
    breadths = jnp.where(image_ids == 0, CW, jnp.where(image_ids == 1, 7 * CW // 9, 5 * CW // 9))
    sizes = jnp.stack(
        [
            jnp.where(turned, breadths, heights),
            jnp.where(turned, heights, breadths),
            turned,
        ],
        axis=1,
    )
    sizes = sizes.reshape(-1).astype(jnp.int32)

    two = 6 * C2 + HID2 + C2
    vec_two = jnp.concatenate([vectors[: 6 * C2], vectors[6 * C2 + HID2 : two]]).reshape(7, C2)
    vec_hid_two = vectors[6 * C2 : 6 * C2 + HID2].reshape(1, HID2)
    wide_end = two + 7 * C3
    vec_three = jnp.concatenate([vectors[two:wide_end], vectors[wide_end + HID3 :]])
    vec_three = jnp.pad(vec_three.reshape(8, C3), ((0, 0), (0, WIDE - C3)))
    vec_hid_three = vectors[wide_end : wide_end + HID3].reshape(1, HID3)

    flips = turned.reshape(-1, 1, 1, 1)
    goal = out_grad.reshape(2 * pairs, H3, W3, C3)
    goal = jnp.where(flips, goal.transpose(0, 2, 1, 3), goal)[:, :LINES]
    goal = goal.reshape(pairs, 2, LINES, W3, C3).transpose(0, 2, 3, 1, 4)
    goal = goal.reshape(pairs, LINES, 2 * W3, C3)
    goal = jnp.pad(goal, ((0, 0), (0, 0), (0, LINE - 2 * W3), (0, WIDE - C3)))
    goal = goal.reshape(pairs, AREA, WIDE)

    state = run_entry(sizes, strips, vec_two)
    result, pixel_back, near, far = run_main(
        (slot_of, near_place, far_place),
        sizes,
        state,
        goal,
        (vec_two, vec_hid_two, vec_three, vec_hid_three),
        pieces,
        strips,
        extra,
    )
    result = result.reshape(pairs, LINES, LINE, WIDE)[:, :, : 2 * W3, :C3]
    result = result.reshape(pairs, LINES, W3, 2, C3).transpose(0, 3, 1, 2, 4)
    result = result.reshape(2 * pairs, LINES, W3, C3)
    result = jnp.pad(result, ((0, 0), (0, H3 - LINES), (0, 0), (0, 0)))
    result = jnp.where(flips, result.transpose(0, 2, 1, 3), result)

    returned = share_out(pixel_back, "tile").astype(f32).reshape(pixels.shape)
    result = result.reshape(out_grad.shape)
    if paired:
        own, *parts = fold_pair(near, swap(far, 1), tile_count // 2)
        pieces = [own] + [swap(part, 2 * k + 2) for k, part in enumerate(parts)]
    else:
        outgoing = jnp.concatenate([near[:half], far[:half]], axis=0)
        outgoing = outgoing.reshape(tile_count, owned + extra, HALF, 128)
        pieces = list(share_out(outgoing, "tile"))
    result, returned, pieces = lax.optimization_barrier((result, returned, pieces))
    own, *parts = fold_tile(spot, pieces, batch_count)
    parts = [
        lax.ppermute(part, "batch", [(i, (i + k + 1) % batch_count) for i in range(batch_count)])
        for k, part in enumerate(parts)
    ]
    quarter, norm = fold_batch(spot, [own] + parts, owned, tile_count)
    quarters = [quarter] + [
        lax.ppermute(quarter, "batch", [(i, (i + k) % batch_count) for i in range(batch_count)])
        for k in range(1, batch_count)
    ]
    norm = share_out(norm, ("batch", "tile"))
    block_grad, left_new, right_new, master_new, weight_copy, whole_vector, clip = update(
        spot, norm, quarters, extra, master, left_stat, right_stat, left_root, right_root
    )
    clip_norm = clip[0, 0]
    share = vectors.shape[0] // tile_count
    whole_vector = whole_vector.reshape(-1)
    vec_grad = lax.dynamic_slice_in_dim(whole_vector, tile_place * share, share, 0)
    vec_moment = moment + vec_grad * vec_grad
    own_vectors = lax.dynamic_slice_in_dim(vectors, tile_place * share, share, 0)
    vec_new = own_vectors - rate_vector * vec_grad / (jnp.sqrt(vec_moment) + eps_adagrad)
    return (
        result,
        returned,
        clip_norm,
        block_grad,
        left_new,
        right_new,
        master_new,
        weight_copy,
        vec_grad,
        vec_moment,
        vec_new,
    )


def solution(mesh):
    placed = (
        P("batch", "tile", None, None, None, None),
        P("batch"),
        P(),
        P("batch", "tile", None, None, None, None, None),
        P("tile", None, None),
        P("tile", None, None),
        P("tile", None, None),
        P("tile", None, None),
        P("tile", None, None),
        P(),
        P("tile"),
    )
    return jax.shard_map(
        on_device,
        mesh=mesh,
        in_specs=placed,
        out_specs=(
            P("batch", "tile", None, None, None, None, None),
            P("batch", "tile", None, None, None, None),
            P(),
            P("tile", None, None),
            P("tile", None, None),
            P("tile", None, None),
            P("tile", None, None),
            P("tile", None, None),
            P("tile"),
            P("tile"),
            P("tile"),
        ),
        check_vma=False,
    )
```

```python
import functools

import jax
import jax.numpy as jnp
from jax import lax
from jax.experimental import pallas as pl
from jax.experimental.pallas import tpu as pltpu
from jax.sharding import PartitionSpec as P

C2 = 128
HID2 = 512
C3 = 320
HID3 = 1280
CH = 36
CW = 36
STRIPS = 4
BS = 64
SR = CH // STRIPS
H3 = CH // 2
W3 = CW // 2
LONG = 7 * CH // 9
LINES = LONG // 2
WIDE = 384
LINE = 40
AREA = LINES * LINE
STEP = 2 * LINE
STEPS = AREA // STEP
HALF = BS // 2

eps_norm = 1e-05
clip_limit = 1.0
rate_matrix = 0.3
rate_vector = 0.3
eps_adagrad = 1e-08
f32 = jnp.float32
bf16 = jnp.bfloat16

SHAPES = [(C2, HID2), (HID2, C2), (9 * C2, C3), (C3, HID3), (HID3, C3)]
USED = sum(rows // BS * (cols // BS) for rows, cols in SHAPES)
VEC_ROWS = (6 * C2 + HID2 + C2 + C3 + 6 * C3 + HID3 + C3) // 128


VEC_BLOCKS = -(-VEC_ROWS // HALF)


def extra_of(owned, groups):
    return VEC_BLOCKS + -(owned + VEC_BLOCKS) % groups


def product(left, right):
    return jnp.dot(left, right, preferred_element_type=f32)


def product_nt(left, right):
    return lax.dot_general(left, right, (((1,), (1,)), ((), ())), preferred_element_type=f32)


def product_tn(left, right):
    return lax.dot_general(left, right, (((0,), (0,)), ((), ())), preferred_element_type=f32)


def gelu_pair(values):
    bell = jnp.exp2(values * values * (-0.5 * 1.4426950408889634))
    step = pl.reciprocal(1.0 + (0.3275911 * 0.7071067811865476) * jnp.abs(values), approx=True)
    tail = step * (
        0.5 * 0.254829592
        + step
        * (
            0.5 * -0.284496736
            + step
            * (0.5 * 1.421413741 + step * (0.5 * -1.453152027 + step * (0.5 * 1.061405429)))
        )
    )
    tail = tail * bell
    share = jnp.where(values >= 0.0, 1.0 - tail, tail)
    return (values * share, share + values * (bell * 0.3989422804014327))


def fold(values):
    chans = values.shape[-1]
    return jnp.sum(values.reshape(-1, 8, chans), axis=0)


def by_image(total):
    total = total + pltpu.roll(total, 4, 0)
    total = total + pltpu.roll(total, 2, 0)
    return jnp.sum(total, axis=1, keepdims=True)


def line(pattern):
    return jnp.concatenate([pattern] * (LINE // 8), axis=0)


def spread(pattern, chans):
    return jnp.broadcast_to(pattern, (8, chans))


def affine(values, factor, shift):
    tiles = values.reshape(-1, 8, values.shape[-1])
    return (tiles * factor + shift).reshape(values.shape)


def scaled(values, factor):
    tiles = values.reshape(-1, 8, values.shape[-1])
    return (tiles * factor).reshape(values.shape)


def from_left(values):
    return pltpu.roll(values, 2, 0)


def from_right(values):
    return pltpu.roll(values, values.shape[0] - 2, 0)


def rounded(values):
    return values.astype(bf16).astype(f32)


def widen(values):
    return jnp.concatenate([values] * (WIDE // 128), axis=-1)


def norm_terms(total, square, count):
    mean = by_image(total) / count
    scaling = lax.rsqrt(by_image(square) / count - mean * mean + eps_norm)
    return (mean, scaling)


def sweep(visit, start):
    return lax.fori_loop(0, STEPS, visit, start, unroll=True)


def step_rows(k, lines=0):
    start = k * STEP + lines * LINE
    return pl.ds(start if isinstance(k, int) else pl.multiple_of(start, LINE), STEP)


def held_in(space, *arrays):
    return [pltpu.with_memory_space_constraint(array, space) for array in arrays]


VMEM_BLOCK = pl.BlockSpec(memory_space=pltpu.VMEM)
HBM = pl.BlockSpec(memory_space=pltpu.HBM)
SMEM = pl.BlockSpec(memory_space=pltpu.SMEM)
ROOMY = pltpu.CompilerParams(vmem_limit_bytes=40 * 1024 * 1024)


class Geometry:
    def __init__(self, size_ref, pair):
        parity = lax.broadcasted_iota(jnp.int32, (8, 128), 0) % 2
        high, broad, turned = (
            jnp.where(parity == 0, size_ref[pair * 6 + n], size_ref[pair * 6 + 3 + n])
            for n in range(3)
        )
        self.high = high
        self.count_two = (high * broad * C2).astype(f32)[:, :1]
        self.high3 = (high + 1) // 2
        broad3 = (broad + 1) // 2
        self.count_three = (self.high3 * broad3 * C3).astype(f32)[:, :1]
        place = lax.broadcasted_iota(jnp.int32, (LINE, 128), 0) // 2
        inside = lax.broadcasted_iota(jnp.int32, (LINE, 128), 0) < 2 * W3
        self.reach = []
        self.col_share = []
        for pc in range(2):
            column = 2 * place + pc
            self.reach.append(jnp.where(inside & (column < line(broad)), line(high), 0))
            edge = (column == 0) | (column == line(broad) - 1)
            self.col_share.append(jnp.where(edge, 0.5, 1.0 / 3.0))
        self.reach3 = jnp.where(inside & (place < line(broad3)), line(self.high3), 0)
        edge3 = (place == 0) | (place == line(broad3) - 1)
        self.col_share3 = jnp.where(edge3, 0.5, 1.0 / 3.0)
        self.flipped = jnp.concatenate([turned] * (STEP // 8), axis=0) > 0

    def share(self, plane, k):
        pr, pc = plane // 2, plane % 2
        return self.lines(4 * k + pr, 2, self.reach[pc], self.col_share[pc], self.high)

    def share3(self, k):
        return self.lines(2 * k, 1, self.reach3, self.col_share3, self.high3)

    def lines(self, row, stride, reach, col_share, height):
        parts = []
        for n in range(2):
            here = row + stride * n
            row_share = jnp.where((here == 0) | (here == height - 1), 0.5, 1.0 / 3.0)
            parts.append(jnp.where(here < reach, line(row_share) * col_share, 0.0))
        return jnp.concatenate(parts, axis=0)


def strip_place(pair, spot, strip_count):
    return lax.rem(pair * 8 + strip_count - 2 + spot, strip_count)


def each_image(size_ref, pair, visit):
    for image in range(2):
        way = size_ref[pair * 6 + 3 * image + 2]
        for flat in (True, False):

            @pl.when(way == (0 if flat else 1))
            def _():
                def one(r, carry):
                    for pr in range(2):
                        for pc in range(2):
                            line_place = pl.ds(r * LINE + image, W3, stride=2)
                            if flat:
                                there = pl.ds((2 * r + pr) * LINE + pc, W3, stride=2)
                            else:
                                there = pl.ds(pc * LINE + 2 * r + pr, W3, stride=2 * LINE)
                            visit(image, pr * 2 + pc, line_place, there)
                    return carry

                lax.fori_loop(0, LINES, one, 0)


def row_windows(col_ref, pc, k):
    both = col_ref[pc, step_rows(k, 1)] + col_ref[2 + pc, step_rows(k, 1)]
    return (both + col_ref[2 + pc, step_rows(k)], both + col_ref[pc, step_rows(k, 2)])


def put_col_windows(col_ref, pr, k, even, odd):
    both = even + odd
    col_ref[pr * 2, step_rows(k, 1)] = both + from_left(odd)
    col_ref[pr * 2 + 1, step_rows(k, 1)] = both + from_right(even)


def clear_edges(col_ref):
    zero_line = jnp.zeros((LINE, C2), f32)
    for plane in range(4):
        col_ref[plane, 0:LINE] = zero_line
        col_ref[plane, AREA + LINE : AREA + 2 * LINE] = zero_line


def entry_kernel(
    pairs,
    strip_count,
    size_ref,
    strips_ref,
    vec_two_ref,
    x_out,
    inv_out,
    pool_out,
    mix_out,
    stat_out,
    image_ref,
    col_ref,
):
    pair = pl.program_id(0) if pairs > 1 else 0
    x_ref, inv_ref, pool_ref, mix_ref = (ref.at[0] for ref in (x_out, inv_out, pool_out, mix_out))
    shape = Geometry(size_ref, pair)
    gain1, bias1, scale1 = (vec_two_ref[n : n + 1] for n in range(3))
    clear_edges(col_ref)

    def to_rows(within, carry):
        for spot in range(2 * STRIPS):
            image, strip = spot // STRIPS, spot % STRIPS
            start = pl.multiple_of((strip * SR + within) * LINE, LINE)
            source = strip_place(pair, spot, strip_count)
            image_ref[image, pl.ds(start, CW)] = strips_ref[source, within].astype(f32)
        return carry

    lax.fori_loop(0, SR, to_rows, 0)

    def take_in(image, plane, line_place, there):
        x_ref[plane, line_place] = image_ref[image, there]

    each_image(size_ref, pair, take_in)

    def arrange(k, carry):
        total, square = carry
        rows = step_rows(k)
        for plane in range(4):
            share = shape.share(plane, k)
            inv_ref[plane, rows] = share
            values = jnp.where(share > 0.0, x_ref[plane, rows], 0.0)
            x_ref[plane, rows] = values
            total = total + fold(values)
            square = square + fold(values * values)
        return (total, square)

    nothing = jnp.zeros((8, C2), f32)
    total, square = sweep(arrange, (nothing, nothing))
    mean1, scaling1 = norm_terms(total, square, shape.count_two)
    factor1 = scaling1 * gain1
    shift1 = bias1 - mean1 * scaling1 * gain1

    def window_cols(k, carry):
        rows = step_rows(k)
        for pr in range(2):
            masked = []
            for pc in range(2):
                plane = pr * 2 + pc
                normal = rounded(affine(x_ref[plane, rows], factor1, shift1))
                masked.append(jnp.where(inv_ref[plane, rows] > 0.0, normal, 0.0))
            put_col_windows(col_ref, pr, k, *masked)
        return carry

    sweep(window_cols, 0)

    def mix(k, carry):
        total, square = carry
        rows = step_rows(k)
        for pc in range(2):
            windows = row_windows(col_ref, pc, k)
            for pr in range(2):
                plane = pr * 2 + pc
                values = x_ref[plane, rows]
                share = inv_ref[plane, rows]
                pooled = windows[pr] * share - rounded(affine(values, factor1, shift1))
                pooled = jnp.where(share > 0.0, pooled, 0.0)
                mixed = values + scale1 * pooled
                pool_ref[plane, rows] = pooled
                mix_ref[plane, rows] = mixed
                total = total + fold(mixed)
                square = square + fold(mixed * mixed)
        return (total, square)

    total, square = sweep(mix, (nothing, nothing))
    mean2, scaling2 = norm_terms(total, square, shape.count_two)
    for n, value in enumerate((mean1, scaling1, mean2, scaling2)):
        stat_out[0, n] = spread(value, 128)


def pair_specs(pairs, shapes, mode=None):
    if pairs == 1:
        return [VMEM_BLOCK] * len(shapes)
    return [
        pl.BlockSpec(
            (1,) + shape, lambda t, rank=len(shape): (t,) + (0,) * rank, pipeline_mode=mode
        )
        for shape in shapes
    ]


def whole_specs(pairs, shapes):
    if pairs == 1:
        return [VMEM_BLOCK] * len(shapes)
    return [
        pl.BlockSpec(
            shape,
            lambda t, rank=len(shape): (0,) * rank,
            pipeline_mode=pl.Buffered(1),
        )
        for shape in shapes
    ]


def pair_arrays(pairs, shapes, kinds):
    make = pltpu.VMEM if pairs == 1 else jax.ShapeDtypeStruct
    return [make((pairs,) + shape, kind) for shape, kind in zip(shapes, kinds)]


STATE = [(4, AREA, C2)] * 4 + [(4, 8, 128)]
BACK = [(4, AREA, C2)] * 2 + [(2, 8, 128)]


def run_entry(sizes, strips, vec_two):
    strip_count = strips.shape[0]
    pairs = strip_count // 8
    return pl.pallas_call(
        functools.partial(entry_kernel, pairs, strip_count),
        grid=() if pairs == 1 else (pairs,),
        in_specs=[SMEM] + whole_specs(pairs, [strips.shape, vec_two.shape]),
        out_specs=pair_specs(pairs, STATE),
        out_shape=pair_arrays(pairs, STATE, [f32] * 5),
        scratch_shapes=[
            pltpu.VMEM((2, CH * LINE, C2), f32),
            pltpu.VMEM((4, AREA + 2 * LINE, C2), f32),
        ],
        compiler_params=ROOMY,
        name="entry",
    )(sizes, strips, vec_two)


def main_kernel(pairs, strip_count, slots, piece_count, *refs):
    fixed, refs = refs[:12], refs[12:]
    inner_kernel(pairs, strip_count, slots, refs[:piece_count], *fixed, *refs[piece_count:])


def inner_kernel(
    pairs,
    strip_count,
    slots,
    piece_refs,
    slot_ref,
    near_place,
    far_place,
    size_ref,
    inv_in,
    mix_in,
    stat_in,
    goal_ref,
    vec_two_ref,
    vec_hid_two_ref,
    vec_three_ref,
    vec_hid_three_ref,
    result_ref,
    zed_out,
    dx_out,
    mean_out,
    near_ref,
    far_ref,
    flat_ref,
    gathered_ref,
    zed_ref,
    hid_ref,
    u_ref,
    g_ref,
    h_ref,
    dy_ref,
    patch_ref,
    dpatch_ref,
    inv3_ref,
    e_ref,
    col3_ref,
    pool3_ref,
    mix3_ref,
    dx3_ref,
    hid3_ref,
    dhid3_ref,
    u3_ref,
    g3_ref,
    h3_ref,
    dy3_ref,
    dpre_ref,
    w1_ref,
    w2_ref,
    we_ref,
    w3_ref,
    w4_ref,
    gw1_ref,
    gw2_ref,
    gwe_ref,
    gw3_ref,
    gw4_ref,
    acc_two,
    acc_hid_two,
    acc_three,
    acc_hid_three,
):
    pair = pl.program_id(0) if pairs > 1 else 0
    weights = [w1_ref, w2_ref, we_ref, w3_ref, w4_ref]
    grads = [gw1_ref, gw2_ref, gwe_ref, gw3_ref, gw4_ref]
    inv_ref, mix_ref, stat_ref = (ref.at[0] for ref in (inv_in, mix_in, stat_in))
    back_ref, dx_ref = zed_out.at[0], dx_out.at[0]
    left_half = lax.broadcasted_iota(jnp.int32, (HALF, 128), 1) < BS

    def at_pair(number, act):
        if pairs == 1:
            act()
        else:
            pl.when(pair == number)(act)

    def begin():
        count = slots // len(piece_refs)
        for n, ref in enumerate(piece_refs):
            gathered_ref[n * count : n * count + count] = ref[...]
        acc_two[...] = jnp.zeros(acc_two.shape, f32)
        acc_hid_two[...] = jnp.zeros(acc_hid_two.shape, f32)
        acc_three[...] = jnp.zeros(acc_three.shape, f32)
        acc_hid_three[...] = jnp.zeros(acc_hid_three.shape, f32)
        offset = 0
        for (rows, cols), ref in zip(SHAPES, weights):
            wide = cols // BS
            for rb in range(rows // BS):
                for cb in range(0, wide, 2):
                    number = offset + rb * wide + cb
                    first = gathered_ref[slot_ref[number]]
                    turned = pltpu.roll(first, BS, 1)
                    if cb + 1 < wide:
                        second = gathered_ref[slot_ref[number + 1]]
                        top = jnp.where(left_half, first, pltpu.roll(second, BS, 1))
                        low = jnp.where(left_half, turned, second)
                    else:
                        top = jnp.where(left_half, first, 0.0)
                        low = jnp.where(left_half, turned, 0.0)
                    place = slice(cb * BS, cb * BS + 128)
                    ref[rb * BS : rb * BS + HALF, place] = top
                    ref[rb * BS + HALF : rb * BS + BS, place] = low
            offset += rows // BS * wide
        w3_ref[C3:, :] = jnp.zeros((WIDE - C3, HID3), bf16)

    at_pair(0, begin)
    shape = Geometry(size_ref, pair)
    count_two, count_three, flipped = shape.count_two, shape.count_three, shape.flipped
    nothing = jnp.zeros((8, C2), f32)
    nothing3 = jnp.zeros((8, WIDE), f32)
    gain2, bias2, scale2, out_bias = (vec_two_ref[n : n + 1] for n in range(3, 7))
    embed_bias, gain3, bias3, scale3 = (vec_three_ref[n : n + 1] for n in range(4))
    gain4, bias4, scale4, out_bias3 = (vec_three_ref[n : n + 1] for n in range(4, 8))
    mean2, scaling2 = stat_ref[2], stat_ref[3]
    factor2 = scaling2 * gain2
    shift2 = bias2 - mean2 * scaling2 * gain2
    for plane in range(4):
        zed_ref[plane, 0:LINE] = jnp.zeros((LINE, C2), f32)
    col3_ref[0:LINE] = jnp.zeros((LINE, WIDE), f32)
    col3_ref[AREA + LINE : AREA + 2 * LINE] = jnp.zeros((LINE, WIDE), f32)

    def plane_rows(plane):
        return slice(plane * AREA, plane * AREA + AREA)

    def begin_plane(plane):
        low = affine(mix_ref[plane], factor2, shift2).astype(bf16)
        h_ref[plane_rows(plane)] = low
        hid_ref[plane % 2] = product(low, w1_ref[...])

    begin_plane(0)
    for plane in range(4):
        if plane < 3:
            begin_plane(plane + 1)
        for k in range(STEPS):
            rows = step_rows(k)
            flat = slice(plane * AREA + k * STEP, plane * AREA + k * STEP + STEP)
            for at in range(0, HID2, 128):
                lanes = slice(at, at + 128)
                active, slope = gelu_pair(hid_ref[plane % 2, rows, lanes] + vec_hid_two_ref[:, lanes])
                u_ref[flat, lanes] = active.astype(bf16)
                g_ref[flat, lanes] = slope.astype(bf16)
        out = product(u_ref[plane_rows(plane)], w2_ref[...]) + out_bias
        zed = jnp.where(inv_ref[plane] > 0.0, mix_ref[plane] + scale2 * out, 0.0)
        zed_ref[plane, LINE : LINE + AREA] = rounded(zed)

    def patches(k, carry):
        rows = step_rows(k)
        taps = []
        for ky in range(3):
            pr = (0 if ky == 1 else 1) * 2
            source = step_rows(k, 0 if ky == 0 else 1)
            even = zed_ref[pr, source]
            odd = zed_ref[pr + 1, source]
            taps.append((from_left(odd), even, odd))
        for ky in range(3):
            for kx in range(3):
                at = (3 * ky + kx) * C2
                tap = taps[ky][kx]
                if ky != kx:
                    tap = jnp.where(flipped, taps[kx][ky], tap)
                patch_ref[rows, at : at + C2] = tap.astype(bf16)
        return carry

    sweep(patches, 0)
    e_ref[...] = product(patch_ref[...], we_ref[...])

    def embed(k, carry):
        total, square = carry
        rows = step_rows(k)
        share = shape.share3(k)
        inv3_ref[rows] = share
        out = jnp.where(widen(share) > 0.0, e_ref[rows] + embed_bias, 0.0)
        e_ref[rows] = out
        return (total + fold(out), square + fold(out * out))

    total, square = sweep(embed, (nothing3, nothing3))
    mean3, scaling3 = norm_terms(total, square, count_three)
    factor3 = scaling3 * gain3
    shift3 = bias3 - mean3 * scaling3 * gain3

    def window_cols3(k, carry):
        rows = step_rows(k)
        normal = rounded(affine(e_ref[rows], factor3, shift3))
        masked = jnp.where(widen(inv3_ref[rows]) > 0.0, normal, 0.0)
        col3_ref[step_rows(k, 1)] = masked + from_left(masked) + from_right(masked)
        return carry

    sweep(window_cols3, 0)

    def row_windows3(k):
        return col3_ref[step_rows(k)] + col3_ref[step_rows(k, 1)] + col3_ref[step_rows(k, 2)]

    def mix3(k, carry):
        total, square = carry
        rows = step_rows(k)
        values = e_ref[rows]
        share = widen(inv3_ref[rows])
        pooled = row_windows3(k) * share - rounded(affine(values, factor3, shift3))
        pooled = jnp.where(share > 0.0, pooled, 0.0)
        mixed = values + scale3 * pooled
        pool3_ref[rows] = pooled
        mix3_ref[rows] = mixed
        return (total + fold(mixed), square + fold(mixed * mixed))

    total, square = sweep(mix3, (nothing3, nothing3))
    mean4, scaling4 = norm_terms(total, square, count_three)
    factor4 = scaling4 * gain4
    shift4 = bias4 - mean4 * scaling4 * gain4
    normal4 = (spread(scaling4, WIDE), spread(-mean4 * scaling4, WIDE))

    def prepare3(k, d_bias):
        rows = step_rows(k)
        h3_ref[rows] = affine(mix3_ref[rows], factor4, shift4).astype(bf16)
        goal = goal_ref[0, rows].astype(f32)
        goal = jnp.where(widen(inv3_ref[rows]) > 0.0, goal, 0.0)
        low_goal = (scale4 * goal).astype(bf16)
        dy3_ref[rows] = low_goal
        return d_bias + fold(low_goal.astype(f32))

    acc_three[7] += sweep(prepare3, nothing3)

    def keep(ref, value, place=slice(None)):
        if pairs == 1:
            ref[place] = value.astype(ref.dtype)
        else:

            @pl.when(pair == 0)
            def _():
                ref[place] = value

            @pl.when(pair > 0)
            def _():
                ref[place] += value

    def begin_chunk(at):
        lanes = slice(at, at + 256)
        hid3_ref[:, lanes] = product(h3_ref[...], w3_ref[:, lanes])
        dhid3_ref[:, lanes] = product_nt(dy3_ref[...], w4_ref[lanes])

    begin_chunk(0)
    for at in range(0, HID3, 256):
        if at + 256 < HID3:
            begin_chunk(at + 256)
        for lane in (at, at + 128):
            lanes = slice(lane, lane + 128)
            total = nothing
            for k in range(STEPS):
                rows = step_rows(k)
                active, slope = gelu_pair(hid3_ref[rows, lanes] + vec_hid_three_ref[:, lanes])
                u3_ref[rows, lanes] = active.astype(bf16)
                low = (slope * dhid3_ref[rows, lanes]).astype(bf16)
                g3_ref[rows, lanes] = low
                total = total + fold(low.astype(f32))
            acc_hid_three[:, lanes] += total
        lanes = slice(at, at + 256)
        out = product(u3_ref[:, lanes], w4_ref[lanes])
        d_low = product_nt(g3_ref[:, lanes], w3_ref[:, lanes])
        result_ref[0] = out if at == 0 else result_ref[0] + out
        dx3_ref[...] = d_low if at == 0 else dx3_ref[...] + d_low
        keep(gw3_ref, product_tn(h3_ref[...], g3_ref[:, lanes]), (slice(None), lanes))
        keep(gw4_ref, product_tn(u3_ref[:, lanes], dy3_ref[...]), lanes)

    def finish3(k, carry):
        d_scale, d_shift, d_gain = carry
        rows = step_rows(k)
        valid = widen(inv3_ref[rows]) > 0.0
        mixed = mix3_ref[rows]
        out = jnp.where(valid, result_ref[0, rows] + out_bias3, 0.0)
        result_ref[0, rows] = mixed + scale4 * out
        d_scale = d_scale + fold(out * goal_ref[0, rows].astype(f32))
        d_low = dx3_ref[rows]
        normal = affine(mixed, *normal4)
        return (d_scale, d_shift + fold(d_low), d_gain + fold(d_low * normal))

    d_scale, d_shift, d_gain = sweep(finish3, (nothing3, nothing3, nothing3))
    acc_three[6] += d_scale
    acc_three[5] += d_shift
    acc_three[4] += d_gain
    mean_shift = by_image(d_shift * gain4) / count_three
    mean_gain = by_image(d_gain * gain4) / count_three
    back_gain4 = scaling4 * gain4
    back_mean4 = spread(-scaling4 * mean_shift, WIDE)
    back_normal4 = spread(scaling4 * mean_gain, WIDE)

    def unmix3(k, d_scale):
        rows = step_rows(k)
        share = widen(inv3_ref[rows])
        valid = share > 0.0
        normal = affine(mix3_ref[rows], *normal4)
        back = affine(dx3_ref[rows], back_gain4, back_mean4) - scaled(normal, back_normal4)
        d_mixed = jnp.where(valid, back + goal_ref[0, rows].astype(f32), 0.0)
        dx3_ref[rows] = d_mixed
        d_scale = d_scale + fold(pool3_ref[rows] * d_mixed)
        weighted = scale3 * d_mixed * share
        col3_ref[step_rows(k, 1)] = weighted + from_left(weighted) + from_right(weighted)
        return d_scale

    acc_three[3] += sweep(unmix3, nothing3)
    normal3 = (spread(scaling3, WIDE), spread(-mean3 * scaling3, WIDE))

    def unpool3(k, carry):
        d_shift, d_gain = carry
        rows = step_rows(k)
        valid = widen(inv3_ref[rows]) > 0.0
        d_normal = jnp.where(valid, row_windows3(k) - scale3 * dx3_ref[rows], 0.0)
        pool3_ref[rows] = d_normal
        normal = affine(e_ref[rows], *normal3)
        return (d_shift + fold(d_normal), d_gain + fold(d_normal * normal))

    d_shift, d_gain = sweep(unpool3, (nothing3, nothing3))
    acc_three[2] += d_shift
    acc_three[1] += d_gain
    mean_shift = by_image(d_shift * gain3) / count_three
    mean_gain = by_image(d_gain * gain3) / count_three
    back_gain3 = scaling3 * gain3
    back_mean3 = spread(-scaling3 * mean_shift, WIDE)
    back_normal3 = spread(scaling3 * mean_gain, WIDE)

    def unnorm3(k, d_bias):
        rows = step_rows(k)
        valid = widen(inv3_ref[rows]) > 0.0
        normal = affine(e_ref[rows], *normal3)
        back = affine(pool3_ref[rows], back_gain3, back_mean3) - scaled(normal, back_normal3)
        low = jnp.where(valid, dx3_ref[rows] + back, 0.0).astype(bf16)
        dpre_ref[rows] = low
        return d_bias + fold(low.astype(f32))

    acc_three[0] += sweep(unnorm3, nothing3)
    keep(gwe_ref, product_tn(patch_ref[...], dpre_ref[...]))
    dpatch_ref[0:AREA] = product_nt(dpre_ref[...], we_ref[...])
    dpatch_ref[AREA : AREA + LINE] = jnp.zeros((LINE, 9 * C2), f32)

    def gather_back(k, carry):
        rows = step_rows(k)

        def tap(ky, kx, source):
            at = (3 * ky + kx) * C2
            value = dpatch_ref[source, at : at + C2]
            if ky != kx:
                at = (3 * kx + ky) * C2
                value = jnp.where(flipped, dpatch_ref[source, at : at + C2], value)
            return value

        sources = []
        for ky in range(3):
            source = step_rows(k, 1 if ky == 0 else 0)
            sources.append(
                (tap(ky, 1, source), tap(ky, 2, source) + from_right(tap(ky, 0, source)))
            )
        for pc in range(2):
            for pr, value in ((0, sources[1][pc]), (1, sources[2][pc] + sources[0][pc])):
                plane = pr * 2 + pc
                valid = inv_ref[plane, rows] > 0.0
                back_ref[plane, rows] = jnp.where(valid, rounded(value), 0.0)
        return carry

    sweep(gather_back, 0)

    normal2 = (spread(scaling2, C2), spread(-mean2 * scaling2, C2))

    def begin_back(plane):
        low_goal = (scale2 * back_ref[plane]).astype(bf16)
        dy_ref[plane_rows(plane)] = low_goal
        hid_ref[plane % 2] = product_nt(low_goal, w2_ref[...])
        return fold(low_goal.astype(f32))

    d_out_bias = begin_back(0)
    d_shift, d_gain = nothing, nothing
    sums = [nothing] * (HID2 // 128)
    new_gw1, new_gw2 = None, None
    for plane in range(4):
        if plane < 3:
            d_out_bias = d_out_bias + begin_back(plane + 1)
        for k in range(STEPS):
            rows = step_rows(k)
            part = slice(plane * AREA + k * STEP, plane * AREA + k * STEP + STEP)
            for n, at in enumerate(range(0, HID2, 128)):
                lanes = slice(at, at + 128)
                low = g_ref[part, lanes].astype(f32) * hid_ref[plane % 2, rows, lanes]
                low = low.astype(bf16)
                g_ref[part, lanes] = low
                sums[n] = sums[n] + fold(low.astype(f32))
        flat = plane_rows(plane)
        d_low = product_nt(g_ref[flat], w1_ref[...])
        dx_ref[plane] = d_low
        d_shift = d_shift + fold(d_low)
        d_gain = d_gain + fold(d_low * affine(mix_ref[plane], *normal2))
        part_gw1 = product_tn(h_ref[flat], g_ref[flat])
        part_gw2 = product_tn(dy_ref[flat], u_ref[flat])
        new_gw1 = part_gw1 if plane == 0 else new_gw1 + part_gw1
        new_gw2 = part_gw2 if plane == 0 else new_gw2 + part_gw2
    new_gw2 = new_gw2.T
    for n, value in enumerate(sums):
        acc_hid_two[:, n * 128 : n * 128 + 128] += value
    acc_two[6] += d_out_bias
    acc_two[4] += d_shift
    acc_two[3] += d_gain
    mean_out[0, 0] = spread(by_image(d_shift * gain2) / count_two, 128)
    mean_out[0, 1] = spread(by_image(d_gain * gain2) / count_two, 128)
    keep(gw1_ref, new_gw1)
    keep(gw2_ref, new_gw2)
    d_scale = fold(w2_ref[...].astype(f32) * new_gw2) + out_bias * d_out_bias
    acc_two[5] += d_scale / scale2

    def finish():
        def put_block(number, block):
            near_ref[near_place[number]] = block
            far_ref[far_place[number]] = block

        offset = 0
        for (rows, cols), ref in zip(SHAPES, grads):
            wide = cols // BS
            for rb in range(rows // BS):
                for cb in range(0, wide, 2):
                    number = offset + rb * wide + cb
                    at = slice(cb * BS, cb * BS + 128)
                    top = ref[rb * BS : rb * BS + HALF, at].astype(bf16)
                    low = ref[rb * BS + HALF : rb * BS + BS, at].astype(bf16)
                    put_block(number, jnp.where(left_half, top, pltpu.roll(low, BS, 1)))
                    if cb + 1 < wide:
                        put_block(number + 1, jnp.where(left_half, pltpu.roll(top, BS, 1), low))
            offset += rows // BS * wide

        def filler(number, carry):
            put_block(number, jnp.zeros((HALF, 128), bf16))
            return carry

        lax.fori_loop(USED, slots, filler, 0)

        flat_ref[...] = jnp.zeros(flat_ref.shape, f32)

        def put(at, total, length):
            if at % 128:
                room = jnp.zeros((8, 128), f32)
                if total.shape[1] < length + BS:
                    total = jnp.concatenate([total, room], axis=1)
                total = pltpu.roll(total, BS, 1)
            whole = jnp.sum(total, axis=0, keepdims=True)
            done = -(at % 128)
            row = at // 128
            lane = 0
            while done < length:
                first = max(0, -done)
                last = min(128, length - done)
                flat_ref[row : row + 1, first:last] = whole[:, lane + first : lane + last]
                done += 128
                lane += 128
                row += 1

        at = 3 * C2
        for n in range(3, 6):
            put(at, acc_two[n], C2)
            at += C2
        put(at, acc_hid_two[...], HID2)
        at += HID2
        put(at, acc_two[6], C2)
        at += C2
        for n in range(7):
            put(at, acc_three[n], C3)
            at += C3
        put(at, acc_hid_three[...], HID3)
        at += HID3
        put(at, acc_three[7], C3)

    at_pair(pairs - 1, finish)


def run_main(places, sizes, state, goal, vectors, pieces, strip_count):
    pairs = goal.shape[0]
    slots = sum(piece.shape[0] for piece in pieces)
    half = slots // 2 + 1
    if pairs == 1:
        pieces = held_in(pltpu.VMEM, *pieces)
        state = held_in(pltpu.VMEM, *state)
    _, inv, _, mix, stat = state
    state_shapes = [STATE[1], STATE[3], STATE[4]]
    grad_kind = bf16 if pairs == 1 else f32
    wide_f32 = pltpu.VMEM((AREA, WIDE), f32)
    wide_bf16 = pltpu.VMEM((AREA, WIDE), bf16)
    scratch = [
        pltpu.VMEM((slots, HALF, 128), bf16),
        pltpu.VMEM((4, AREA + LINE, C2), f32),
        pltpu.VMEM((2, AREA, HID2), f32),
        pltpu.VMEM((4 * AREA, HID2), bf16),
        pltpu.VMEM((4 * AREA, HID2), bf16),
        pltpu.VMEM((4 * AREA, C2), bf16),
        pltpu.VMEM((4 * AREA, C2), bf16),
        pltpu.VMEM((AREA, 9 * C2), bf16),
        pltpu.VMEM((AREA + LINE, 9 * C2), f32),
        pltpu.VMEM((AREA, 128), f32),
        wide_f32,
        pltpu.VMEM((AREA + 2 * LINE, WIDE), f32),
        wide_f32,
        wide_f32,
        wide_f32,
        pltpu.VMEM((AREA, HID3), f32),
        pltpu.VMEM((AREA, HID3), f32),
        pltpu.VMEM((AREA, HID3), bf16),
        pltpu.VMEM((AREA, HID3), bf16),
        wide_bf16,
        wide_bf16,
        wide_bf16,
        pltpu.VMEM((C2, HID2), bf16),
        pltpu.VMEM((HID2, C2), bf16),
        pltpu.VMEM((9 * C2, WIDE), bf16),
        pltpu.VMEM((WIDE, HID3), bf16),
        pltpu.VMEM((HID3, WIDE), bf16),
        pltpu.VMEM((C2, HID2), grad_kind),
        pltpu.VMEM((HID2, C2), grad_kind),
        pltpu.VMEM((9 * C2, WIDE), grad_kind),
        pltpu.VMEM((WIDE, HID3), grad_kind),
        pltpu.VMEM((HID3, WIDE), grad_kind),
        pltpu.VMEM((7, 8, C2), f32),
        pltpu.VMEM((8, HID2), f32),
        pltpu.VMEM((8, 8, WIDE), f32),
        pltpu.VMEM((8, HID3), f32),
    ]
    out_shapes = [(half, HALF, 128), (half, HALF, 128), (VEC_BLOCKS * HALF, 128)]
    make = pltpu.VMEM if pairs == 1 else jax.ShapeDtypeStruct
    return pl.pallas_call(
        functools.partial(main_kernel, pairs, strip_count, slots, len(pieces)),
        grid=() if pairs == 1 else (pairs,),
        in_specs=[SMEM] * 4
        + pair_specs(pairs, state_shapes + [goal.shape[1:]], pl.Buffered(1))
        + whole_specs(pairs, [array.shape for array in (*vectors, *pieces)]),
        out_specs=pair_specs(pairs, [(AREA, WIDE)] + BACK) + whole_specs(pairs, out_shapes),
        out_shape=pair_arrays(pairs, [(AREA, WIDE)] + BACK, [f32] * 4)
        + [make(shape, kind) for shape, kind in zip(out_shapes, (bf16, bf16, f32))],
        scratch_shapes=scratch,
        compiler_params=pltpu.CompilerParams(
            vmem_limit_bytes=(46 if pairs == 1 else 60) * 1024 * 1024,
            fuse_transposed_lhs_in_matmul=True,
        ),
        name="blocks",
    )(*places, sizes, inv, mix, stat, goal, *vectors, *pieces)


def exit_kernel(
    pairs,
    strip_count,
    size_ref,
    x_in,
    inv_in,
    pool_in,
    mix_in,
    stat_in,
    zed_in,
    dx_in,
    mean_in,
    flat_ref,
    vec_two_ref,
    payload_hbm,
    payload_ref,
    image_ref,
    col_ref,
    dx_ref,
    back_ref,
    acc_ref,
    flat_ref_out,
    sem,
):
    pair = pl.program_id(0) if pairs > 1 else 0
    x_ref, inv_ref, pool_ref, mix_ref, stat_ref, zed_ref, low_ref, mean_ref = (
        ref.at[0] for ref in (x_in, inv_in, pool_in, mix_in, stat_in, zed_in, dx_in, mean_in)
    )
    shape = Geometry(size_ref, pair)
    count_two = shape.count_two
    gain1, bias1, scale1, gain2 = (vec_two_ref[n : n + 1] for n in range(4))
    mean1, scaling1, mean2, scaling2 = (stat_ref[n] for n in range(4))
    normal2 = (scaling2, -mean2 * scaling2)
    clear_edges(col_ref)
    nothing = jnp.zeros((8, C2), f32)
    back_gain2 = scaling2 * gain2
    back_mean2 = -scaling2 * mean_ref[0]
    back_normal2 = scaling2 * mean_ref[1]

    if pairs > 1:

        @pl.when(pair == 0)
        def _():
            acc_ref[...] = jnp.zeros(acc_ref.shape, f32)

    def add_up(n, total):
        acc_ref[n] = total if pairs == 1 else acc_ref[n] + total

    def unmix(k, d_scale):
        rows = step_rows(k)
        for pr in range(2):
            weighted = []
            for pc in range(2):
                plane = pr * 2 + pc
                share = inv_ref[plane, rows]
                normal = affine(mix_ref[plane, rows], *normal2)
                back = affine(low_ref[plane, rows], back_gain2, back_mean2)
                back = back - scaled(normal, back_normal2)
                d_mixed = jnp.where(share > 0.0, zed_ref[plane, rows] + back, 0.0)
                dx_ref[plane, rows] = d_mixed
                d_scale = d_scale + fold(pool_ref[plane, rows] * d_mixed)
                weighted.append(scale1 * d_mixed * share)
            put_col_windows(col_ref, pr, k, *weighted)
        return d_scale

    add_up(2, sweep(unmix, nothing))
    normal1 = (spread(scaling1, C2), spread(-mean1 * scaling1, C2))

    def unpool(k, carry):
        d_shift, d_gain = carry
        rows = step_rows(k)
        for pc in range(2):
            windows = row_windows(col_ref, pc, k)
            for pr in range(2):
                plane = pr * 2 + pc
                valid = inv_ref[plane, rows] > 0.0
                d_normal = windows[pr] - scale1 * dx_ref[plane, rows]
                d_normal = jnp.where(valid, d_normal, 0.0)
                back_ref[plane, rows] = d_normal
                normal = affine(x_ref[plane, rows], *normal1)
                d_shift = d_shift + fold(d_normal)
                d_gain = d_gain + fold(d_normal * normal)
        return (d_shift, d_gain)

    d_shift, d_gain = sweep(unpool, (nothing, nothing))
    add_up(1, d_shift)
    add_up(0, d_gain)
    mean_shift = by_image(d_shift * gain1) / count_two
    mean_gain = by_image(d_gain * gain1) / count_two
    back_gain1 = scaling1 * gain1
    back_mean1 = spread(-scaling1 * mean_shift, C2)
    back_normal1 = spread(scaling1 * mean_gain, C2)

    def unnorm(k, carry):
        rows = step_rows(k)
        for plane in range(4):
            normal = affine(x_ref[plane, rows], *normal1)
            back = affine(back_ref[plane, rows], back_gain1, back_mean1)
            back = back - scaled(normal, back_normal1)
            valid = inv_ref[plane, rows] > 0.0
            dx_ref[plane, rows] = jnp.where(valid, dx_ref[plane, rows] + back, 0.0)
        return carry

    sweep(unnorm, 0)

    def give_back(image, plane, line_place, there):
        image_ref[image, there] = dx_ref[plane, line_place]

    image_ref[...] = jnp.zeros(image_ref.shape, f32)
    each_image(size_ref, pair, give_back)

    def from_rows(within, carry):
        for spot in range(2 * STRIPS):
            image, strip = spot // STRIPS, spot % STRIPS
            start = pl.multiple_of((strip * SR + within) * LINE, LINE)
            target = strip_place(pair, spot, strip_count)
            payload_ref[target, within] = image_ref[image, pl.ds(start, CW)].astype(bf16)
        return carry

    lax.fori_loop(0, SR, from_rows, 0)

    def finish():
        flat_ref_out[...] = flat_ref[...]
        for n in range(3):
            flat = jnp.sum(acc_ref[n], axis=0, keepdims=True)
            flat_ref_out[n : n + 1] = flat
        packed = flat_ref_out[...].astype(bf16)
        for n in range(VEC_BLOCKS):

            def leave(target, carry):
                payload_ref[target, SR + n, 0:HALF] = packed[n * HALF : (n + 1) * HALF]
                return carry

            lax.fori_loop(0, strip_count, leave, 0)
        copy = pltpu.make_async_copy(payload_ref, payload_hbm, sem)
        copy.start()
        copy.wait()

    if pairs == 1:
        finish()
    else:
        pl.when(pair == pairs - 1)(finish)


def run_exit(sizes, state, back, flat, vec_two, strip_count):
    pairs = strip_count // 8
    payload = (strip_count, SR + VEC_BLOCKS, CW, C2)
    plane_f32 = pltpu.VMEM((4, AREA, C2), f32)
    arrays = [*state, *back]
    if pairs == 1:
        arrays = held_in(pltpu.VMEM, *arrays)
    return pl.pallas_call(
        functools.partial(exit_kernel, pairs, strip_count),
        grid=() if pairs == 1 else (pairs,),
        in_specs=[SMEM]
        + pair_specs(pairs, STATE + BACK, pl.Buffered(1))
        + whole_specs(pairs, [flat.shape, vec_two.shape]),
        out_specs=HBM,
        out_shape=pltpu.HBM(payload, bf16),
        scratch_shapes=[
            pltpu.VMEM(payload, bf16),
            pltpu.VMEM((2, CH * LINE, C2), f32),
            pltpu.VMEM((4, AREA + 2 * LINE, C2), f32),
            plane_f32,
            plane_f32,
            pltpu.VMEM((3, 8, C2), f32),
            pltpu.VMEM(flat.shape, f32),
            pltpu.SemaphoreType.DMA,
        ],
        compiler_params=ROOMY,
        name="exit",
    )(sizes, *arrays, flat, vec_two)


def pack_kernel(master_ref, dense_ref):
    values = master_ref[...]
    dense_ref[...] = jnp.concatenate([values[:, :HALF], values[:, HALF:]], axis=2).astype(bf16)


def pack(master):
    owned = master.shape[0]
    return pl.pallas_call(
        pack_kernel,
        out_shape=jax.ShapeDtypeStruct((owned, HALF, 2 * BS), bf16),
        name="pack",
    )(master)


def fold_pair_kernel(near_ref, got_ref, own_ref, *part_refs):
    share = own_ref.shape[0]

    def one(n, carry):
        for k in range(len(part_refs) + 1):
            total = near_ref[k * share + n].astype(f32) + got_ref[k * share + n].astype(f32)
            if k == 0:
                own_ref[n] = total
            else:
                part_refs[k - 1][n] = total.astype(bf16)
        return carry

    lax.fori_loop(0, share, one, 0, unroll=4)


def fold_pair(near, got, groups):
    shape = ((near.shape[0] - 1) // groups,) + near.shape[1:]
    return pl.pallas_call(
        fold_pair_kernel,
        in_specs=[VMEM_BLOCK] * 2,
        out_specs=[VMEM_BLOCK] * groups,
        out_shape=[pltpu.VMEM(shape, f32)] + [pltpu.VMEM(shape, bf16)] * (groups - 1),
        compiler_params=ROOMY,
        name="fold_pair",
    )(*held_in(pltpu.VMEM, near, got))


def fold_tile_kernel(pieces, spot_ref, vector_ref, *refs):
    piece_refs, refs = refs[:pieces], refs[pieces:]
    out_refs, sum_ref = refs[:-1], refs[-1]
    groups = len(out_refs)
    share = out_refs[0].shape[0]
    owned = piece_refs[0].shape[0]
    extra = sum_ref.shape[0]
    for n in range(extra):
        total = jnp.zeros((HALF, 128), f32)
        if n < vector_ref.shape[1]:
            for target in range(vector_ref.shape[0]):
                total = total + vector_ref[target, n].astype(f32)
        sum_ref[n] = total

    def one(n, carry):
        for k, out_ref in enumerate(out_refs):
            number = lax.rem(spot_ref[0] + k, groups) * share + n
            block = jnp.minimum(number, owned - 1)
            total = piece_refs[0][block].astype(f32)
            for ref in piece_refs[1:]:
                total = total + ref[block].astype(f32)
            rest = sum_ref[jnp.maximum(number - owned, 0)]
            out_ref[n] = jnp.where(number < owned, total, rest).astype(out_ref.dtype)
        return carry

    lax.fori_loop(0, share, one, 0, unroll=share <= 16)


def fold_tile(spot, pieces, vector, extra, groups):
    shape = ((pieces[0].shape[0] + extra) // groups,) + pieces[0].shape[1:]
    return pl.pallas_call(
        functools.partial(fold_tile_kernel, len(pieces)),
        in_specs=[SMEM] + [VMEM_BLOCK] * (len(pieces) + 1),
        out_specs=[VMEM_BLOCK] * groups,
        out_shape=[pltpu.VMEM(shape, f32)] + [pltpu.VMEM(shape, bf16)] * (groups - 1),
        scratch_shapes=[pltpu.VMEM((extra, HALF, 128), f32)],
        compiler_params=ROOMY,
        name="fold_tile",
    )(spot, *held_in(pltpu.VMEM, vector, *pieces))


def fold_batch_kernel(owned, vector_weight, spot_ref, *refs):
    part_refs, (total_ref, norm_ref) = refs[:-2], refs[-2:]
    share = total_ref.shape[0]
    square = jnp.zeros((8, 128), f32)
    for n in range(share):
        total = part_refs[0][n].astype(f32)
        for ref in part_refs[1:]:
            total = total + ref[n].astype(f32)
        total_ref[n] = total.astype(bf16)
        weight = jnp.where(spot_ref[0] * share + n < owned, 1.0, vector_weight)
        square = square + weight * fold(total * total)
    square = jnp.sum(jnp.sum(square, axis=1, keepdims=True), axis=0, keepdims=True)
    norm_ref[...] = jnp.broadcast_to(square[None], norm_ref.shape)


def fold_batch(spot, parts, owned, tile_count):
    count = tile_count * len(parts)
    return pl.pallas_call(
        functools.partial(fold_batch_kernel, owned, 1.0 / tile_count),
        in_specs=[SMEM] + [VMEM_BLOCK] * len(parts),
        out_specs=[VMEM_BLOCK] * 2,
        out_shape=[pltpu.VMEM(parts[0].shape, bf16), pltpu.VMEM((count, 1, 128), f32)],
        name="fold_batch",
    )(spot, *held_in(pltpu.VMEM, *parts))


def update_kernel(owned, groups, spot_ref, norm_ref, *refs):
    quarters, refs = refs[:groups], refs[groups:]
    stat_hbm, out_hbm, (vector_ref, clip_ref), refs = refs[:5], refs[5:10], refs[10:12], refs[12:]
    stat_refs, out_refs, (in_sem, out_sem) = refs[:5], refs[5:10], refs[10:]
    master_ref, left_stat_ref, right_stat_ref, left_root_ref, right_root_ref = stat_refs
    grad_ref, left_ref, right_ref, new_ref, copy_ref = out_refs
    share = quarters[0].shape[0]
    spans = [(first, min(8, owned - first)) for first in range(0, owned, 8)]

    def copies_of(sources, targets, sems):
        return [
            [
                pltpu.make_async_copy(
                    source.at[pl.ds(*span)], target.at[pl.ds(*span)], sems.at[5 * n + k]
                )
                for k, (source, target) in enumerate(zip(sources, targets))
            ]
            for n, span in enumerate(spans)
        ]

    copies_in = copies_of(stat_hbm, stat_refs, in_sem)
    copies_out = copies_of(out_refs, out_hbm, out_sem)
    for copies in copies_in:
        for copy in copies:
            copy.start()
    norm = jnp.sqrt(jnp.sum(norm_ref[...], axis=0))
    factor = jnp.minimum(1.0, clip_limit / norm)
    left_half = lax.broadcasted_iota(jnp.int32, (HALF, 128), 1) < BS

    def summed(number):
        source = number // share
        local = number - source * share
        turn = lax.rem(spot_ref[0] - source + groups, groups)
        value = quarters[0][local].astype(f32)
        for k in range(1, groups):
            value = jnp.where(turn == k, quarters[k][local].astype(f32), value)
        return value * factor

    def one_group(first, count):
        sides = []
        for n in range(first, first + count, 2):
            dense = summed(n)
            turned = pltpu.roll(dense, BS, 1)
            if n + 1 < first + count:
                second = summed(n + 1)
                top = jnp.where(left_half, dense, pltpu.roll(second, BS, 1))
                low = jnp.where(left_half, turned, second)
                side = jnp.concatenate([top, low], axis=0)
                grad_ref[n + 1] = pltpu.roll(side, BS, 1)[:, :BS]
            else:
                side = jnp.concatenate([dense, turned], axis=0)[:, :BS]
            grad_ref[n] = side[:, :BS]
            sides.append(side.astype(bf16))
        wide = jnp.concatenate(sides, axis=1)
        order = count * BS
        row_block = lax.broadcasted_iota(jnp.int32, (order, order), 0) // BS
        col_block = lax.broadcasted_iota(jnp.int32, (order, order), 1) // BS
        diagonal = row_block == col_block
        here = pl.ds(first, count)
        tall = jnp.where(diagonal, jnp.concatenate([wide] * count, axis=0), 0.0)
        left = product_nt(tall, wide).reshape(count, BS, BS)
        left_ref[here] = 0.5 * left_stat_ref[here] + 0.5 * left
        right = product_tn(wide, wide)
        for n in range(count):
            at = n // 2 * 128
            block = right[n * BS : n * BS + BS, at : min(at + 128, order)]
            if n % 2:
                block = pltpu.roll(block, BS, 1)
            right_ref[first + n] = 0.5 * right_stat_ref[first + n] + 0.5 * block[:, :BS]
        roots = left_root_ref[here].reshape(order, BS).astype(bf16)
        stepped = jnp.where(diagonal, product(roots, wide), 0.0).astype(bf16)
        roots = right_root_ref[here].reshape(order, BS).astype(bf16)
        stepped = product(stepped, roots).reshape(count, BS, BS)
        new = master_ref[here] - rate_matrix * stepped
        new_ref[here] = new
        copy_ref[here] = new.astype(bf16)

    clip_ref[...] = norm
    for n in range(vector_ref.shape[0]):
        vector_ref[n] = summed(owned + n)
    for (first, count), arriving, leaving in zip(spans, copies_in, copies_out):
        for copy in arriving:
            copy.wait()
        for start in range(first, first + count, 4):
            one_group(start, min(4, first + count - start))
        for copy in leaving:
            copy.start()
    for leaving in copies_out:
        for copy in leaving:
            copy.wait()


def update(spot, norm, quarters, extra, *stats):
    shape = stats[0].shape
    groups = len(quarters)
    types = [f32] * 4 + [bf16]
    steps = -(-shape[0] // 8)
    return pl.pallas_call(
        functools.partial(update_kernel, shape[0], groups),
        in_specs=[SMEM] + [VMEM_BLOCK] * (groups + 1) + [HBM] * 5,
        out_specs=[HBM] * 5 + [VMEM_BLOCK] * 2,
        out_shape=[pltpu.HBM(shape, kind) for kind in types]
        + [
            jax.ShapeDtypeStruct((extra, HALF, 128), f32),
            jax.ShapeDtypeStruct((1, 128), f32),
        ],
        scratch_shapes=[pltpu.VMEM(shape, f32)] * 5
        + [pltpu.VMEM(shape, kind) for kind in types]
        + [
            pltpu.SemaphoreType.DMA((5 * steps,)),
            pltpu.SemaphoreType.DMA((5 * steps,)),
        ],
        compiler_params=ROOMY,
        name="update",
    )(spot, *held_in(pltpu.VMEM, norm, *quarters), *held_in(pltpu.HBM, *stats))


def share_out(pieces, axis):
    return lax.all_to_all(pieces, axis, split_axis=0, concat_axis=0, tiled=True)


def swap(piece, distance):
    count = lax.axis_size("tile")
    return lax.ppermute(piece, "tile", [(i, i ^ distance) for i in range(count)])


def on_device(
    pixels,
    buckets,
    slot_owner_table,
    out_grad,
    master,
    left_stat,
    right_stat,
    left_root,
    right_root,
    vectors,
    moment,
):
    tile_count = lax.axis_size("tile")
    tile_place = lax.axis_index("tile")
    slot_count = pixels.shape[2]
    group_count = tile_count // STRIPS
    pairs = group_count // 2
    owned = master.shape[0]
    slots = owned * tile_count
    batch_count = lax.axis_size("batch")
    spot = lax.axis_index("batch").astype(jnp.int32).reshape(1)
    extra = extra_of(owned, batch_count)
    strips = share_out(pixels.reshape((tile_count,) + pixels.shape[3:]), "tile")
    strips, dense = lax.optimization_barrier((strips, pack(master)))
    paired = tile_count <= 8
    if paired:
        mine = [dense] + [swap(dense, 2 * k) for k in range(1, tile_count // 2)]
        pieces = mine + [swap(piece, 1) for piece in mine]
    else:
        pieces = [lax.all_gather(dense, "tile", axis=0, tiled=True)]

    numbers = jnp.arange(slots, dtype=jnp.int32)
    slot_of = jnp.sum(
        jnp.where(slot_owner_table[None, :] == numbers[:, None], numbers[None, :], 0), axis=1
    )
    owner = slot_of // owned
    within = slot_of - owner * owned
    place_of = slot_of
    if paired:
        apart = owner ^ tile_place
        apart = (apart & 1) * (tile_count // 2) + (apart >> 1)
        slot_of = place_of = within + owned * apart
    half = slots // 2
    near_place = jnp.where(place_of < half, place_of, half)
    far_place = jnp.where(place_of < half, half, place_of - half)
    image_ids = lax.dynamic_index_in_dim(
        buckets.reshape(group_count, slot_count), tile_place, 1, keepdims=False
    )
    turned = image_ids >= 2
    heights = jnp.where(image_ids == 0, 5 * CH // 9, jnp.where(image_ids == 1, 7 * CH // 9, CH))
    breadths = jnp.where(image_ids == 0, CW, jnp.where(image_ids == 1, 7 * CW // 9, 5 * CW // 9))
    sizes = jnp.stack(
        [
            jnp.where(turned, breadths, heights),
            jnp.where(turned, heights, breadths),
            turned,
        ],
        axis=1,
    )
    sizes = sizes.reshape(-1).astype(jnp.int32)

    two = 6 * C2 + HID2 + C2
    vec_two = jnp.concatenate([vectors[: 6 * C2], vectors[6 * C2 + HID2 : two]]).reshape(7, C2)
    vec_hid_two = vectors[6 * C2 : 6 * C2 + HID2].reshape(1, HID2)
    wide_end = two + 7 * C3
    vec_three = jnp.concatenate([vectors[two:wide_end], vectors[wide_end + HID3 :]])
    vec_three = jnp.pad(vec_three.reshape(8, C3), ((0, 0), (0, WIDE - C3)))
    vec_hid_three = vectors[wide_end : wide_end + HID3].reshape(1, HID3)

    flips = turned.reshape(-1, 1, 1, 1)
    goal = out_grad.reshape(2 * pairs, H3, W3, C3)
    goal = jnp.where(flips, goal.transpose(0, 2, 1, 3), goal)[:, :LINES]
    goal = goal.reshape(pairs, 2, LINES, W3, C3).transpose(0, 2, 3, 1, 4)
    goal = goal.reshape(pairs, LINES, 2 * W3, C3)
    goal = jnp.pad(goal, ((0, 0), (0, 0), (0, LINE - 2 * W3), (0, WIDE - C3)))
    goal = goal.reshape(pairs, AREA, WIDE)

    state = run_entry(sizes, strips, vec_two)
    result, *back, near, far, flat = run_main(
        (slot_of, near_place, far_place),
        sizes,
        state,
        goal,
        (vec_two, vec_hid_two, vec_three, vec_hid_three),
        pieces,
        tile_count,
    )
    payload = run_exit(sizes, state, back, flat, vec_two, tile_count)
    if paired:
        own, *parts = fold_pair(near, swap(far, 1), tile_count // 2)
        result, payload, *parts = lax.optimization_barrier((result, payload, *parts))
        pieces = [own] + [swap(part, 2 * k + 2) for k, part in enumerate(parts)]
    else:
        outgoing = jnp.concatenate([near[:half], far[:half]], axis=0)
        pieces = list(share_out(outgoing.reshape(tile_count, owned, HALF, 128), "tile"))
    payload = share_out(payload, "tile")
    returned = payload[:, :SR].astype(f32).reshape(pixels.shape)
    vector = payload[:, SR:, :HALF]
    result = result.reshape(pairs, LINES, LINE, WIDE)[:, :, : 2 * W3, :C3]
    result = result.reshape(pairs, LINES, W3, 2, C3).transpose(0, 3, 1, 2, 4)
    result = result.reshape(2 * pairs, LINES, W3, C3)
    result = jnp.pad(result, ((0, 0), (0, H3 - LINES), (0, 0), (0, 0)))
    result = jnp.where(flips, result.transpose(0, 2, 1, 3), result)

    result = result.reshape(out_grad.shape)
    result, returned, vector = lax.optimization_barrier((result, returned, vector))
    own, *parts = fold_tile(spot, pieces, vector, extra, batch_count)
    parts = [
        lax.ppermute(part, "batch", [(i, (i + k + 1) % batch_count) for i in range(batch_count)])
        for k, part in enumerate(parts)
    ]
    quarter, norm = fold_batch(spot, [own] + parts, owned, tile_count)
    quarters = [quarter] + [
        lax.ppermute(quarter, "batch", [(i, (i + k) % batch_count) for i in range(batch_count)])
        for k in range(1, batch_count)
    ]
    norm = share_out(norm, ("batch", "tile"))
    block_grad, left_new, right_new, master_new, weight_copy, whole_vector, clip = update(
        spot, norm, quarters, extra, master, left_stat, right_stat, left_root, right_root
    )
    clip_norm = clip[0, 0]
    share = vectors.shape[0] // tile_count
    whole_vector = whole_vector.reshape(-1)
    vec_grad = lax.dynamic_slice_in_dim(whole_vector, tile_place * share, share, 0)
    vec_moment = moment + vec_grad * vec_grad
    own_vectors = lax.dynamic_slice_in_dim(vectors, tile_place * share, share, 0)
    vec_new = own_vectors - rate_vector * vec_grad / (jnp.sqrt(vec_moment) + eps_adagrad)
    return (
        result,
        returned,
        clip_norm,
        block_grad,
        left_new,
        right_new,
        master_new,
        weight_copy,
        vec_grad,
        vec_moment,
        vec_new,
    )


def solution(mesh):
    placed = (
        P("batch", "tile", None, None, None, None),
        P("batch"),
        P(),
        P("batch", "tile", None, None, None, None, None),
        P("tile", None, None),
        P("tile", None, None),
        P("tile", None, None),
        P("tile", None, None),
        P("tile", None, None),
        P(),
        P("tile"),
    )
    return jax.shard_map(
        on_device,
        mesh=mesh,
        in_specs=placed,
        out_specs=(
            P("batch", "tile", None, None, None, None, None),
            P("batch", "tile", None, None, None, None),
            P(),
            P("tile", None, None),
            P("tile", None, None),
            P("tile", None, None),
            P("tile", None, None),
            P("tile", None, None),
            P("tile"),
            P("tile"),
            P("tile"),
        ),
        check_vma=False,
    )
```

```python
import functools

import jax
import jax.numpy as jnp
from jax import lax
from jax.experimental import pallas as pl
from jax.experimental.pallas import tpu as pltpu
from jax.sharding import PartitionSpec as P

C2 = 128
HID2 = 512
C3 = 320
HID3 = 1280
CH = 36
CW = 36
STRIPS = 4
BS = 64
SR = CH // STRIPS
H3 = CH // 2
W3 = CW // 2
LONG = 7 * CH // 9
LINES = LONG // 2
WIDE = 384
LINE = 40
AREA = LINES * LINE
STEP = 2 * LINE
STEPS = AREA // STEP
HALF = BS // 2

eps_norm = 1e-05
clip_limit = 1.0
rate_matrix = 0.3
rate_vector = 0.3
eps_adagrad = 1e-08
f32 = jnp.float32
bf16 = jnp.bfloat16

SHAPES = [(C2, HID2), (HID2, C2), (9 * C2, C3), (C3, HID3), (HID3, C3)]
USED = sum(rows // BS * (cols // BS) for rows, cols in SHAPES)
VEC_ROWS = (6 * C2 + HID2 + C2 + C3 + 6 * C3 + HID3 + C3) // 128


VEC_BLOCKS = -(-VEC_ROWS // HALF)


def extra_of(owned, groups):
    return VEC_BLOCKS + -(owned + VEC_BLOCKS) % groups


def product(left, right):
    return jnp.dot(left, right, preferred_element_type=f32)


def product_nt(left, right):
    return lax.dot_general(left, right, (((1,), (1,)), ((), ())), preferred_element_type=f32)


def product_tn(left, right):
    return lax.dot_general(left, right, (((0,), (0,)), ((), ())), preferred_element_type=f32)


def gelu_pair(values):
    bell = jnp.exp2(values * values * (-0.5 * 1.4426950408889634))
    step = pl.reciprocal(1.0 + (0.3275911 * 0.7071067811865476) * jnp.abs(values), approx=True)
    tail = step * (
        0.5 * 0.254829592
        + step
        * (
            0.5 * -0.284496736
            + step
            * (0.5 * 1.421413741 + step * (0.5 * -1.453152027 + step * (0.5 * 1.061405429)))
        )
    )
    tail = tail * bell
    share = jnp.where(values >= 0.0, 1.0 - tail, tail)
    return (values * share, share + values * (bell * 0.3989422804014327))


def fold(values):
    chans = values.shape[-1]
    return jnp.sum(values.reshape(-1, 8, chans), axis=0)


def by_image(total):
    total = total + pltpu.roll(total, 4, 0)
    total = total + pltpu.roll(total, 2, 0)
    return jnp.sum(total, axis=1, keepdims=True)


def line(pattern):
    return jnp.concatenate([pattern] * (LINE // 8), axis=0)


def spread(pattern, chans):
    return jnp.broadcast_to(pattern, (8, chans))


def affine(values, factor, shift):
    tiles = values.reshape(-1, 8, values.shape[-1])
    return (tiles * factor + shift).reshape(values.shape)


def scaled(values, factor):
    tiles = values.reshape(-1, 8, values.shape[-1])
    return (tiles * factor).reshape(values.shape)


def from_left(values):
    return pltpu.roll(values, 2, 0)


def from_right(values):
    return pltpu.roll(values, values.shape[0] - 2, 0)


def rounded(values):
    return values.astype(bf16).astype(f32)


def widen(values):
    return jnp.concatenate([values] * (WIDE // 128), axis=-1)


def norm_terms(total, square, count):
    mean = by_image(total) / count
    scaling = lax.rsqrt(by_image(square) / count - mean * mean + eps_norm)
    return (mean, scaling)


def sweep(visit, start):
    return lax.fori_loop(0, STEPS, visit, start, unroll=True)


def step_rows(k, lines=0):
    start = k * STEP + lines * LINE
    return pl.ds(start if isinstance(k, int) else pl.multiple_of(start, LINE), STEP)


def held_in(space, *arrays):
    return [pltpu.with_memory_space_constraint(array, space) for array in arrays]


VMEM_BLOCK = pl.BlockSpec(memory_space=pltpu.VMEM)
HBM = pl.BlockSpec(memory_space=pltpu.HBM)
SMEM = pl.BlockSpec(memory_space=pltpu.SMEM)
ROOMY = pltpu.CompilerParams(vmem_limit_bytes=40 * 1024 * 1024)


class Geometry:
    def __init__(self, size_ref, pair):
        parity = lax.broadcasted_iota(jnp.int32, (8, 128), 0) % 2
        high, broad, turned = (
            jnp.where(parity == 0, size_ref[pair * 6 + n], size_ref[pair * 6 + 3 + n])
            for n in range(3)
        )
        self.high = high
        self.count_two = (high * broad * C2).astype(f32)[:, :1]
        self.high3 = (high + 1) // 2
        broad3 = (broad + 1) // 2
        self.count_three = (self.high3 * broad3 * C3).astype(f32)[:, :1]
        place = lax.broadcasted_iota(jnp.int32, (LINE, 128), 0) // 2
        inside = lax.broadcasted_iota(jnp.int32, (LINE, 128), 0) < 2 * W3
        self.reach = []
        self.col_share = []
        for pc in range(2):
            column = 2 * place + pc
            self.reach.append(jnp.where(inside & (column < line(broad)), line(high), 0))
            edge = (column == 0) | (column == line(broad) - 1)
            self.col_share.append(jnp.where(edge, 0.5, 1.0 / 3.0))
        self.reach3 = jnp.where(inside & (place < line(broad3)), line(self.high3), 0)
        edge3 = (place == 0) | (place == line(broad3) - 1)
        self.col_share3 = jnp.where(edge3, 0.5, 1.0 / 3.0)
        self.flipped = jnp.concatenate([turned] * (STEP // 8), axis=0) > 0

    def share(self, plane, k):
        pr, pc = plane // 2, plane % 2
        return self.lines(4 * k + pr, 2, self.reach[pc], self.col_share[pc], self.high)

    def share3(self, k):
        return self.lines(2 * k, 1, self.reach3, self.col_share3, self.high3)

    def lines(self, row, stride, reach, col_share, height):
        parts = []
        for n in range(2):
            here = row + stride * n
            row_share = jnp.where((here == 0) | (here == height - 1), 0.5, 1.0 / 3.0)
            parts.append(jnp.where(here < reach, line(row_share) * col_share, 0.0))
        return jnp.concatenate(parts, axis=0)


def strip_place(pair, spot, strip_count):
    return lax.rem(pair * 8 + strip_count - 2 + spot, strip_count)


def each_image(size_ref, pair, visit):
    for image in range(2):
        way = size_ref[pair * 6 + 3 * image + 2]
        for flat in (True, False):

            @pl.when(way == (0 if flat else 1))
            def _():
                def one(r, carry):
                    for pr in range(2):
                        for pc in range(2):
                            line_place = pl.ds(r * LINE + image, W3, stride=2)
                            if flat:
                                there = pl.ds((2 * r + pr) * LINE + pc, W3, stride=2)
                            else:
                                there = pl.ds(pc * LINE + 2 * r + pr, W3, stride=2 * LINE)
                            visit(image, pr * 2 + pc, line_place, there)
                    return carry

                lax.fori_loop(0, LINES, one, 0)


def row_windows(col_ref, pc, k):
    both = col_ref[pc, step_rows(k, 1)] + col_ref[2 + pc, step_rows(k, 1)]
    return (both + col_ref[2 + pc, step_rows(k)], both + col_ref[pc, step_rows(k, 2)])


def put_col_windows(col_ref, pr, k, even, odd):
    both = even + odd
    col_ref[pr * 2, step_rows(k, 1)] = both + from_left(odd)
    col_ref[pr * 2 + 1, step_rows(k, 1)] = both + from_right(even)


def clear_edges(col_ref):
    zero_line = jnp.zeros((LINE, C2), f32)
    for plane in range(4):
        col_ref[plane, 0:LINE] = zero_line
        col_ref[plane, AREA + LINE : AREA + 2 * LINE] = zero_line


def entry_kernel(
    pairs,
    strip_count,
    size_ref,
    strips_ref,
    vec_two_ref,
    x_out,
    inv_out,
    pool_out,
    mix_out,
    stat_out,
    image_ref,
    col_ref,
):
    pair = pl.program_id(0) if pairs > 1 else 0
    x_ref, inv_ref, pool_ref, mix_ref = (ref.at[0] for ref in (x_out, inv_out, pool_out, mix_out))
    shape = Geometry(size_ref, pair)
    gain1, bias1, scale1 = (vec_two_ref[n : n + 1] for n in range(3))
    clear_edges(col_ref)

    def to_rows(within, carry):
        for spot in range(2 * STRIPS):
            image, strip = spot // STRIPS, spot % STRIPS
            start = pl.multiple_of((strip * SR + within) * LINE, LINE)
            source = strip_place(pair, spot, strip_count)
            image_ref[image, pl.ds(start, CW)] = strips_ref[source, within].astype(f32)
        return carry

    lax.fori_loop(0, SR, to_rows, 0)

    def take_in(image, plane, line_place, there):
        x_ref[plane, line_place] = image_ref[image, there]

    each_image(size_ref, pair, take_in)

    def arrange(k, carry):
        total, square = carry
        rows = step_rows(k)
        for plane in range(4):
            share = shape.share(plane, k)
            inv_ref[plane, rows] = share
            values = jnp.where(share > 0.0, x_ref[plane, rows], 0.0)
            x_ref[plane, rows] = values
            total = total + fold(values)
            square = square + fold(values * values)
        return (total, square)

    nothing = jnp.zeros((8, C2), f32)
    total, square = sweep(arrange, (nothing, nothing))
    mean1, scaling1 = norm_terms(total, square, shape.count_two)
    factor1 = scaling1 * gain1
    shift1 = bias1 - mean1 * scaling1 * gain1

    def window_cols(k, carry):
        rows = step_rows(k)
        for pr in range(2):
            masked = []
            for pc in range(2):
                plane = pr * 2 + pc
                normal = rounded(affine(x_ref[plane, rows], factor1, shift1))
                masked.append(jnp.where(inv_ref[plane, rows] > 0.0, normal, 0.0))
            put_col_windows(col_ref, pr, k, *masked)
        return carry

    sweep(window_cols, 0)

    def mix(k, carry):
        total, square = carry
        rows = step_rows(k)
        for pc in range(2):
            windows = row_windows(col_ref, pc, k)
            for pr in range(2):
                plane = pr * 2 + pc
                values = x_ref[plane, rows]
                share = inv_ref[plane, rows]
                pooled = windows[pr] * share - rounded(affine(values, factor1, shift1))
                pooled = jnp.where(share > 0.0, pooled, 0.0)
                mixed = values + scale1 * pooled
                pool_ref[plane, rows] = pooled
                mix_ref[plane, rows] = mixed
                total = total + fold(mixed)
                square = square + fold(mixed * mixed)
        return (total, square)

    total, square = sweep(mix, (nothing, nothing))
    mean2, scaling2 = norm_terms(total, square, shape.count_two)
    for n, value in enumerate((mean1, scaling1, mean2, scaling2)):
        stat_out[0, n] = spread(value, 128)


def pair_specs(pairs, shapes, mode=None):
    if pairs == 1:
        return [VMEM_BLOCK] * len(shapes)
    return [
        pl.BlockSpec(
            (1,) + shape, lambda t, rank=len(shape): (t,) + (0,) * rank, pipeline_mode=mode
        )
        for shape in shapes
    ]


def whole_specs(pairs, shapes):
    if pairs == 1:
        return [VMEM_BLOCK] * len(shapes)
    return [
        pl.BlockSpec(
            shape,
            lambda t, rank=len(shape): (0,) * rank,
            pipeline_mode=pl.Buffered(1),
        )
        for shape in shapes
    ]


def pair_arrays(pairs, shapes, kinds):
    make = pltpu.VMEM if pairs == 1 else jax.ShapeDtypeStruct
    return [make((pairs,) + shape, kind) for shape, kind in zip(shapes, kinds)]


STATE = [(4, AREA, C2)] * 4 + [(4, 8, 128)]
BACK = [(4, AREA, C2)] * 2 + [(2, 8, 128)]


def run_entry(sizes, strips, vec_two):
    strip_count = strips.shape[0]
    pairs = strip_count // 8
    return pl.pallas_call(
        functools.partial(entry_kernel, pairs, strip_count),
        grid=() if pairs == 1 else (pairs,),
        in_specs=[SMEM] + whole_specs(pairs, [strips.shape, vec_two.shape]),
        out_specs=pair_specs(pairs, STATE),
        out_shape=pair_arrays(pairs, STATE, [f32] * 5),
        scratch_shapes=[
            pltpu.VMEM((2, CH * LINE, C2), f32),
            pltpu.VMEM((4, AREA + 2 * LINE, C2), f32),
        ],
        compiler_params=ROOMY,
        name="entry",
    )(sizes, strips, vec_two)


def main_kernel(pairs, strip_count, slots, piece_count, *refs):
    fixed, refs = refs[:12], refs[12:]
    inner_kernel(pairs, strip_count, slots, refs[:piece_count], *fixed, *refs[piece_count:])


def inner_kernel(
    pairs,
    strip_count,
    slots,
    piece_refs,
    slot_ref,
    near_place,
    far_place,
    size_ref,
    inv_in,
    mix_in,
    stat_in,
    goal_ref,
    vec_two_ref,
    vec_hid_two_ref,
    vec_three_ref,
    vec_hid_three_ref,
    result_ref,
    zed_out,
    dx_out,
    mean_out,
    near_ref,
    far_ref,
    flat_ref,
    gathered_ref,
    zed_ref,
    hid_ref,
    u_ref,
    g_ref,
    h_ref,
    dy_ref,
    patch_ref,
    dpatch_ref,
    inv3_ref,
    e_ref,
    col3_ref,
    pool3_ref,
    mix3_ref,
    dx3_ref,
    hid3_ref,
    dhid3_ref,
    u3_ref,
    g3_ref,
    h3_ref,
    dy3_ref,
    dpre_ref,
    w1_ref,
    w2_ref,
    we_ref,
    w3_ref,
    w4_ref,
    gw1_ref,
    gw2_ref,
    gwe_ref,
    gw3_ref,
    gw4_ref,
    acc_two,
    acc_hid_two,
    acc_three,
    acc_hid_three,
):
    pair = pl.program_id(0) if pairs > 1 else 0
    weights = [w1_ref, w2_ref, we_ref, w3_ref, w4_ref]
    grads = [gw1_ref, gw2_ref, gwe_ref, gw3_ref, gw4_ref]
    inv_ref, mix_ref, stat_ref = (ref.at[0] for ref in (inv_in, mix_in, stat_in))
    back_ref, dx_ref = zed_out.at[0], dx_out.at[0]
    left_half = lax.broadcasted_iota(jnp.int32, (HALF, 128), 1) < BS

    def at_pair(number, act):
        if pairs == 1:
            act()
        else:
            pl.when(pair == number)(act)

    def begin():
        count = slots // len(piece_refs)
        for n, ref in enumerate(piece_refs):
            gathered_ref[n * count : n * count + count] = ref[...]
        acc_two[...] = jnp.zeros(acc_two.shape, f32)
        acc_hid_two[...] = jnp.zeros(acc_hid_two.shape, f32)
        acc_three[...] = jnp.zeros(acc_three.shape, f32)
        acc_hid_three[...] = jnp.zeros(acc_hid_three.shape, f32)
        offset = 0
        for (rows, cols), ref in zip(SHAPES, weights):
            wide = cols // BS
            for rb in range(rows // BS):
                for cb in range(0, wide, 2):
                    number = offset + rb * wide + cb
                    first = gathered_ref[slot_ref[number]]
                    turned = pltpu.roll(first, BS, 1)
                    if cb + 1 < wide:
                        second = gathered_ref[slot_ref[number + 1]]
                        top = jnp.where(left_half, first, pltpu.roll(second, BS, 1))
                        low = jnp.where(left_half, turned, second)
                    else:
                        top = jnp.where(left_half, first, 0.0)
                        low = jnp.where(left_half, turned, 0.0)
                    place = slice(cb * BS, cb * BS + 128)
                    ref[rb * BS : rb * BS + HALF, place] = top
                    ref[rb * BS + HALF : rb * BS + BS, place] = low
            offset += rows // BS * wide
        w3_ref[C3:, :] = jnp.zeros((WIDE - C3, HID3), bf16)

    at_pair(0, begin)
    shape = Geometry(size_ref, pair)
    count_two, count_three, flipped = shape.count_two, shape.count_three, shape.flipped
    nothing = jnp.zeros((8, C2), f32)
    nothing3 = jnp.zeros((8, WIDE), f32)
    gain2, bias2, scale2, out_bias = (vec_two_ref[n : n + 1] for n in range(3, 7))
    embed_bias, gain3, bias3, scale3 = (vec_three_ref[n : n + 1] for n in range(4))
    gain4, bias4, scale4, out_bias3 = (vec_three_ref[n : n + 1] for n in range(4, 8))
    mean2, scaling2 = stat_ref[2], stat_ref[3]
    factor2 = scaling2 * gain2
    shift2 = bias2 - mean2 * scaling2 * gain2
    for plane in range(4):
        zed_ref[plane, 0:LINE] = jnp.zeros((LINE, C2), f32)
    col3_ref[0:LINE] = jnp.zeros((LINE, WIDE), f32)
    col3_ref[AREA + LINE : AREA + 2 * LINE] = jnp.zeros((LINE, WIDE), f32)

    def plane_rows(plane):
        return slice(plane * AREA, plane * AREA + AREA)

    def begin_plane(plane):
        low = affine(mix_ref[plane], factor2, shift2).astype(bf16)
        h_ref[plane_rows(plane)] = low
        hid_ref[plane % 2] = product(low, w1_ref[...])

    begin_plane(0)
    for plane in range(4):
        if plane < 3:
            begin_plane(plane + 1)
        for k in range(STEPS):
            rows = step_rows(k)
            flat = slice(plane * AREA + k * STEP, plane * AREA + k * STEP + STEP)
            for at in range(0, HID2, 128):
                lanes = slice(at, at + 128)
                active, slope = gelu_pair(hid_ref[plane % 2, rows, lanes] + vec_hid_two_ref[:, lanes])
                u_ref[flat, lanes] = active.astype(bf16)
                g_ref[flat, lanes] = slope.astype(bf16)
        out = product(u_ref[plane_rows(plane)], w2_ref[...]) + out_bias
        zed = jnp.where(inv_ref[plane] > 0.0, mix_ref[plane] + scale2 * out, 0.0)
        zed_ref[plane, LINE : LINE + AREA] = rounded(zed)

    def patches(k, carry):
        rows = step_rows(k)
        taps = []
        for ky in range(3):
            pr = (0 if ky == 1 else 1) * 2
            source = step_rows(k, 0 if ky == 0 else 1)
            even = zed_ref[pr, source]
            odd = zed_ref[pr + 1, source]
            taps.append((from_left(odd), even, odd))
        for ky in range(3):
            for kx in range(3):
                at = (3 * ky + kx) * C2
                tap = taps[ky][kx]
                if ky != kx:
                    tap = jnp.where(flipped, taps[kx][ky], tap)
                patch_ref[rows, at : at + C2] = tap.astype(bf16)
        return carry

    sweep(patches, 0)
    e_ref[...] = product(patch_ref[...], we_ref[...])

    def embed(k, carry):
        total, square = carry
        rows = step_rows(k)
        share = shape.share3(k)
        inv3_ref[rows] = share
        out = jnp.where(widen(share) > 0.0, e_ref[rows] + embed_bias, 0.0)
        e_ref[rows] = out
        return (total + fold(out), square + fold(out * out))

    total, square = sweep(embed, (nothing3, nothing3))
    mean3, scaling3 = norm_terms(total, square, count_three)
    factor3 = scaling3 * gain3
    shift3 = bias3 - mean3 * scaling3 * gain3

    def window_cols3(k, carry):
        rows = step_rows(k)
        normal = rounded(affine(e_ref[rows], factor3, shift3))
        masked = jnp.where(widen(inv3_ref[rows]) > 0.0, normal, 0.0)
        col3_ref[step_rows(k, 1)] = masked + from_left(masked) + from_right(masked)
        return carry

    sweep(window_cols3, 0)

    def row_windows3(k):
        return col3_ref[step_rows(k)] + col3_ref[step_rows(k, 1)] + col3_ref[step_rows(k, 2)]

    def mix3(k, carry):
        total, square = carry
        rows = step_rows(k)
        values = e_ref[rows]
        share = widen(inv3_ref[rows])
        pooled = row_windows3(k) * share - rounded(affine(values, factor3, shift3))
        pooled = jnp.where(share > 0.0, pooled, 0.0)
        mixed = values + scale3 * pooled
        pool3_ref[rows] = pooled
        mix3_ref[rows] = mixed
        return (total + fold(mixed), square + fold(mixed * mixed))

    total, square = sweep(mix3, (nothing3, nothing3))
    mean4, scaling4 = norm_terms(total, square, count_three)
    factor4 = scaling4 * gain4
    shift4 = bias4 - mean4 * scaling4 * gain4
    normal4 = (spread(scaling4, WIDE), spread(-mean4 * scaling4, WIDE))

    def prepare3(k, d_bias):
        rows = step_rows(k)
        h3_ref[rows] = affine(mix3_ref[rows], factor4, shift4).astype(bf16)
        goal = goal_ref[0, rows].astype(f32)
        goal = jnp.where(widen(inv3_ref[rows]) > 0.0, goal, 0.0)
        low_goal = (scale4 * goal).astype(bf16)
        dy3_ref[rows] = low_goal
        return d_bias + fold(low_goal.astype(f32))

    acc_three[7] += sweep(prepare3, nothing3)

    def keep(ref, value, place=slice(None)):
        if pairs == 1:
            ref[place] = value.astype(ref.dtype)
        else:

            @pl.when(pair == 0)
            def _():
                ref[place] = value

            @pl.when(pair > 0)
            def _():
                ref[place] += value

    def begin_chunk(at):
        lanes = slice(at, at + 256)
        hid3_ref[:, lanes] = product(h3_ref[...], w3_ref[:, lanes])
        dhid3_ref[:, lanes] = product_nt(dy3_ref[...], w4_ref[lanes])

    begin_chunk(0)
    for at in range(0, HID3, 256):
        if at + 256 < HID3:
            begin_chunk(at + 256)
        for lane in (at, at + 128):
            lanes = slice(lane, lane + 128)
            total = nothing
            for k in range(STEPS):
                rows = step_rows(k)
                active, slope = gelu_pair(hid3_ref[rows, lanes] + vec_hid_three_ref[:, lanes])
                u3_ref[rows, lanes] = active.astype(bf16)
                low = (slope * dhid3_ref[rows, lanes]).astype(bf16)
                g3_ref[rows, lanes] = low
                total = total + fold(low.astype(f32))
            acc_hid_three[:, lanes] += total
        lanes = slice(at, at + 256)
        out = product(u3_ref[:, lanes], w4_ref[lanes])
        d_low = product_nt(g3_ref[:, lanes], w3_ref[:, lanes])
        result_ref[0] = out if at == 0 else result_ref[0] + out
        dx3_ref[...] = d_low if at == 0 else dx3_ref[...] + d_low
        keep(gw3_ref, product_tn(h3_ref[...], g3_ref[:, lanes]), (slice(None), lanes))
        keep(gw4_ref, product_tn(u3_ref[:, lanes], dy3_ref[...]), lanes)

    def finish3(k, carry):
        d_scale, d_shift, d_gain = carry
        rows = step_rows(k)
        valid = widen(inv3_ref[rows]) > 0.0
        mixed = mix3_ref[rows]
        out = jnp.where(valid, result_ref[0, rows] + out_bias3, 0.0)
        result_ref[0, rows] = mixed + scale4 * out
        d_scale = d_scale + fold(out * goal_ref[0, rows].astype(f32))
        d_low = dx3_ref[rows]
        normal = affine(mixed, *normal4)
        return (d_scale, d_shift + fold(d_low), d_gain + fold(d_low * normal))

    d_scale, d_shift, d_gain = sweep(finish3, (nothing3, nothing3, nothing3))
    acc_three[6] += d_scale
    acc_three[5] += d_shift
    acc_three[4] += d_gain
    mean_shift = by_image(d_shift * gain4) / count_three
    mean_gain = by_image(d_gain * gain4) / count_three
    back_gain4 = scaling4 * gain4
    back_mean4 = spread(-scaling4 * mean_shift, WIDE)
    back_normal4 = spread(scaling4 * mean_gain, WIDE)

    def unmix3(k, d_scale):
        rows = step_rows(k)
        share = widen(inv3_ref[rows])
        valid = share > 0.0
        normal = affine(mix3_ref[rows], *normal4)
        back = affine(dx3_ref[rows], back_gain4, back_mean4) - scaled(normal, back_normal4)
        d_mixed = jnp.where(valid, back + goal_ref[0, rows].astype(f32), 0.0)
        dx3_ref[rows] = d_mixed
        d_scale = d_scale + fold(pool3_ref[rows] * d_mixed)
        weighted = scale3 * d_mixed * share
        col3_ref[step_rows(k, 1)] = weighted + from_left(weighted) + from_right(weighted)
        return d_scale

    acc_three[3] += sweep(unmix3, nothing3)
    normal3 = (spread(scaling3, WIDE), spread(-mean3 * scaling3, WIDE))

    def unpool3(k, carry):
        d_shift, d_gain = carry
        rows = step_rows(k)
        valid = widen(inv3_ref[rows]) > 0.0
        d_normal = jnp.where(valid, row_windows3(k) - scale3 * dx3_ref[rows], 0.0)
        pool3_ref[rows] = d_normal
        normal = affine(e_ref[rows], *normal3)
        return (d_shift + fold(d_normal), d_gain + fold(d_normal * normal))

    d_shift, d_gain = sweep(unpool3, (nothing3, nothing3))
    acc_three[2] += d_shift
    acc_three[1] += d_gain
    mean_shift = by_image(d_shift * gain3) / count_three
    mean_gain = by_image(d_gain * gain3) / count_three
    back_gain3 = scaling3 * gain3
    back_mean3 = spread(-scaling3 * mean_shift, WIDE)
    back_normal3 = spread(scaling3 * mean_gain, WIDE)

    def unnorm3(k, d_bias):
        rows = step_rows(k)
        valid = widen(inv3_ref[rows]) > 0.0
        normal = affine(e_ref[rows], *normal3)
        back = affine(pool3_ref[rows], back_gain3, back_mean3) - scaled(normal, back_normal3)
        low = jnp.where(valid, dx3_ref[rows] + back, 0.0).astype(bf16)
        dpre_ref[rows] = low
        return d_bias + fold(low.astype(f32))

    acc_three[0] += sweep(unnorm3, nothing3)
    keep(gwe_ref, product_tn(patch_ref[...], dpre_ref[...]))
    dpatch_ref[0:AREA] = product_nt(dpre_ref[...], we_ref[...])
    dpatch_ref[AREA : AREA + LINE] = jnp.zeros((LINE, 9 * C2), f32)

    def gather_back(k, carry):
        rows = step_rows(k)

        def tap(ky, kx, source):
            at = (3 * ky + kx) * C2
            value = dpatch_ref[source, at : at + C2]
            if ky != kx:
                at = (3 * kx + ky) * C2
                value = jnp.where(flipped, dpatch_ref[source, at : at + C2], value)
            return value

        sources = []
        for ky in range(3):
            source = step_rows(k, 1 if ky == 0 else 0)
            sources.append(
                (tap(ky, 1, source), tap(ky, 2, source) + from_right(tap(ky, 0, source)))
            )
        for pc in range(2):
            for pr, value in ((0, sources[1][pc]), (1, sources[2][pc] + sources[0][pc])):
                plane = pr * 2 + pc
                valid = inv_ref[plane, rows] > 0.0
                back_ref[plane, rows] = jnp.where(valid, rounded(value), 0.0)
        return carry

    sweep(gather_back, 0)

    normal2 = (spread(scaling2, C2), spread(-mean2 * scaling2, C2))

    def begin_back(plane):
        low_goal = (scale2 * back_ref[plane]).astype(bf16)
        dy_ref[plane_rows(plane)] = low_goal
        hid_ref[plane % 2] = product_nt(low_goal, w2_ref[...])
        return fold(low_goal.astype(f32))

    d_out_bias = begin_back(0)
    d_shift, d_gain = nothing, nothing
    sums = [nothing] * (HID2 // 128)
    new_gw1, new_gw2 = None, None
    for plane in range(4):
        if plane < 3:
            d_out_bias = d_out_bias + begin_back(plane + 1)
        for k in range(STEPS):
            rows = step_rows(k)
            part = slice(plane * AREA + k * STEP, plane * AREA + k * STEP + STEP)
            for n, at in enumerate(range(0, HID2, 128)):
                lanes = slice(at, at + 128)
                low = g_ref[part, lanes].astype(f32) * hid_ref[plane % 2, rows, lanes]
                low = low.astype(bf16)
                g_ref[part, lanes] = low
                sums[n] = sums[n] + fold(low.astype(f32))
        flat = plane_rows(plane)
        d_low = product_nt(g_ref[flat], w1_ref[...])
        dx_ref[plane] = d_low
        d_shift = d_shift + fold(d_low)
        d_gain = d_gain + fold(d_low * affine(mix_ref[plane], *normal2))
        part_gw1 = product_tn(h_ref[flat], g_ref[flat])
        part_gw2 = product_tn(dy_ref[flat], u_ref[flat])
        new_gw1 = part_gw1 if plane == 0 else new_gw1 + part_gw1
        new_gw2 = part_gw2 if plane == 0 else new_gw2 + part_gw2
    new_gw2 = new_gw2.T
    for n, value in enumerate(sums):
        acc_hid_two[:, n * 128 : n * 128 + 128] += value
    acc_two[6] += d_out_bias
    acc_two[4] += d_shift
    acc_two[3] += d_gain
    mean_out[0, 0] = spread(by_image(d_shift * gain2) / count_two, 128)
    mean_out[0, 1] = spread(by_image(d_gain * gain2) / count_two, 128)
    keep(gw1_ref, new_gw1)
    keep(gw2_ref, new_gw2)
    d_scale = fold(w2_ref[...].astype(f32) * new_gw2) + out_bias * d_out_bias
    acc_two[5] += d_scale / scale2

    def finish():
        def put_block(number, block):
            near_ref[near_place[number]] = block
            far_ref[far_place[number]] = block

        offset = 0
        for (rows, cols), ref in zip(SHAPES, grads):
            wide = cols // BS
            for rb in range(rows // BS):
                for cb in range(0, wide, 2):
                    number = offset + rb * wide + cb
                    at = slice(cb * BS, cb * BS + 128)
                    top = ref[rb * BS : rb * BS + HALF, at].astype(bf16)
                    low = ref[rb * BS + HALF : rb * BS + BS, at].astype(bf16)
                    put_block(number, jnp.where(left_half, top, pltpu.roll(low, BS, 1)))
                    if cb + 1 < wide:
                        put_block(number + 1, jnp.where(left_half, pltpu.roll(top, BS, 1), low))
            offset += rows // BS * wide

        def filler(number, carry):
            put_block(number, jnp.zeros((HALF, 128), bf16))
            return carry

        lax.fori_loop(USED, slots, filler, 0)

        flat_ref[...] = jnp.zeros(flat_ref.shape, f32)

        def put(at, total, length):
            if at % 128:
                room = jnp.zeros((8, 128), f32)
                if total.shape[1] < length + BS:
                    total = jnp.concatenate([total, room], axis=1)
                total = pltpu.roll(total, BS, 1)
            whole = jnp.sum(total, axis=0, keepdims=True)
            done = -(at % 128)
            row = at // 128
            lane = 0
            while done < length:
                first = max(0, -done)
                last = min(128, length - done)
                flat_ref[row : row + 1, first:last] = whole[:, lane + first : lane + last]
                done += 128
                lane += 128
                row += 1

        at = 3 * C2
        for n in range(3, 6):
            put(at, acc_two[n], C2)
            at += C2
        put(at, acc_hid_two[...], HID2)
        at += HID2
        put(at, acc_two[6], C2)
        at += C2
        for n in range(7):
            put(at, acc_three[n], C3)
            at += C3
        put(at, acc_hid_three[...], HID3)
        at += HID3
        put(at, acc_three[7], C3)

    at_pair(pairs - 1, finish)


def run_main(places, sizes, state, goal, vectors, pieces, strip_count):
    pairs = goal.shape[0]
    slots = sum(piece.shape[0] for piece in pieces)
    half = slots // 2 + 1
    if pairs == 1:
        pieces = held_in(pltpu.VMEM, *pieces)
        state = held_in(pltpu.VMEM, *state)
    _, inv, _, mix, stat = state
    state_shapes = [STATE[1], STATE[3], STATE[4]]
    grad_kind = bf16 if pairs == 1 else f32
    wide_f32 = pltpu.VMEM((AREA, WIDE), f32)
    wide_bf16 = pltpu.VMEM((AREA, WIDE), bf16)
    scratch = [
        pltpu.VMEM((slots, HALF, 128), bf16),
        pltpu.VMEM((4, AREA + LINE, C2), f32),
        pltpu.VMEM((2, AREA, HID2), f32),
        pltpu.VMEM((4 * AREA, HID2), bf16),
        pltpu.VMEM((4 * AREA, HID2), bf16),
        pltpu.VMEM((4 * AREA, C2), bf16),
        pltpu.VMEM((4 * AREA, C2), bf16),
        pltpu.VMEM((AREA, 9 * C2), bf16),
        pltpu.VMEM((AREA + LINE, 9 * C2), f32),
        pltpu.VMEM((AREA, 128), f32),
        wide_f32,
        pltpu.VMEM((AREA + 2 * LINE, WIDE), f32),
        wide_f32,
        wide_f32,
        wide_f32,
        pltpu.VMEM((AREA, HID3), f32),
        pltpu.VMEM((AREA, HID3), f32),
        pltpu.VMEM((AREA, HID3), bf16),
        pltpu.VMEM((AREA, HID3), bf16),
        wide_bf16,
        wide_bf16,
        wide_bf16,
        pltpu.VMEM((C2, HID2), bf16),
        pltpu.VMEM((HID2, C2), bf16),
        pltpu.VMEM((9 * C2, WIDE), bf16),
        pltpu.VMEM((WIDE, HID3), bf16),
        pltpu.VMEM((HID3, WIDE), bf16),
        pltpu.VMEM((C2, HID2), grad_kind),
        pltpu.VMEM((HID2, C2), grad_kind),
        pltpu.VMEM((9 * C2, WIDE), grad_kind),
        pltpu.VMEM((WIDE, HID3), grad_kind),
        pltpu.VMEM((HID3, WIDE), grad_kind),
        pltpu.VMEM((7, 8, C2), f32),
        pltpu.VMEM((8, HID2), f32),
        pltpu.VMEM((8, 8, WIDE), f32),
        pltpu.VMEM((8, HID3), f32),
    ]
    out_shapes = [(half, HALF, 128), (half, HALF, 128), (VEC_BLOCKS * HALF, 128)]
    make = pltpu.VMEM if pairs == 1 else jax.ShapeDtypeStruct
    return pl.pallas_call(
        functools.partial(main_kernel, pairs, strip_count, slots, len(pieces)),
        grid=() if pairs == 1 else (pairs,),
        in_specs=[SMEM] * 4
        + pair_specs(pairs, state_shapes + [goal.shape[1:]], pl.Buffered(1))
        + whole_specs(pairs, [array.shape for array in (*vectors, *pieces)]),
        out_specs=pair_specs(pairs, [(AREA, WIDE)] + BACK) + whole_specs(pairs, out_shapes),
        out_shape=pair_arrays(pairs, [(AREA, WIDE)] + BACK, [f32] * 4)
        + [make(shape, kind) for shape, kind in zip(out_shapes, (bf16, bf16, f32))],
        scratch_shapes=scratch,
        compiler_params=pltpu.CompilerParams(
            vmem_limit_bytes=(46 if pairs == 1 else 60) * 1024 * 1024,
            fuse_transposed_lhs_in_matmul=True,
        ),
        name="blocks",
    )(*places, sizes, inv, mix, stat, goal, *vectors, *pieces)


def exit_kernel(
    pairs,
    strip_count,
    size_ref,
    x_in,
    inv_in,
    pool_in,
    mix_in,
    stat_in,
    zed_in,
    dx_in,
    mean_in,
    flat_ref,
    vec_two_ref,
    payload_hbm,
    vector_ref,
    payload_ref,
    image_ref,
    col_ref,
    dx_ref,
    back_ref,
    acc_ref,
    sem,
):
    pair = pl.program_id(0) if pairs > 1 else 0
    x_ref, inv_ref, pool_ref, mix_ref, stat_ref, zed_ref, low_ref, mean_ref = (
        ref.at[0] for ref in (x_in, inv_in, pool_in, mix_in, stat_in, zed_in, dx_in, mean_in)
    )
    shape = Geometry(size_ref, pair)
    count_two = shape.count_two
    gain1, bias1, scale1, gain2 = (vec_two_ref[n : n + 1] for n in range(4))
    mean1, scaling1, mean2, scaling2 = (stat_ref[n] for n in range(4))
    normal2 = (scaling2, -mean2 * scaling2)
    clear_edges(col_ref)
    nothing = jnp.zeros((8, C2), f32)
    back_gain2 = scaling2 * gain2
    back_mean2 = -scaling2 * mean_ref[0]
    back_normal2 = scaling2 * mean_ref[1]

    if pairs > 1:

        @pl.when(pair == 0)
        def _():
            acc_ref[...] = jnp.zeros(acc_ref.shape, f32)

    def add_up(n, total):
        acc_ref[n] = total if pairs == 1 else acc_ref[n] + total

    def unmix(k, d_scale):
        rows = step_rows(k)
        for pr in range(2):
            weighted = []
            for pc in range(2):
                plane = pr * 2 + pc
                share = inv_ref[plane, rows]
                normal = affine(mix_ref[plane, rows], *normal2)
                back = affine(low_ref[plane, rows], back_gain2, back_mean2)
                back = back - scaled(normal, back_normal2)
                d_mixed = jnp.where(share > 0.0, zed_ref[plane, rows] + back, 0.0)
                dx_ref[plane, rows] = d_mixed
                d_scale = d_scale + fold(pool_ref[plane, rows] * d_mixed)
                weighted.append(scale1 * d_mixed * share)
            put_col_windows(col_ref, pr, k, *weighted)
        return d_scale

    add_up(2, sweep(unmix, nothing))
    normal1 = (spread(scaling1, C2), spread(-mean1 * scaling1, C2))

    def unpool(k, carry):
        d_shift, d_gain = carry
        rows = step_rows(k)
        for pc in range(2):
            windows = row_windows(col_ref, pc, k)
            for pr in range(2):
                plane = pr * 2 + pc
                valid = inv_ref[plane, rows] > 0.0
                d_normal = windows[pr] - scale1 * dx_ref[plane, rows]
                d_normal = jnp.where(valid, d_normal, 0.0)
                back_ref[plane, rows] = d_normal
                normal = affine(x_ref[plane, rows], *normal1)
                d_shift = d_shift + fold(d_normal)
                d_gain = d_gain + fold(d_normal * normal)
        return (d_shift, d_gain)

    d_shift, d_gain = sweep(unpool, (nothing, nothing))
    add_up(1, d_shift)
    add_up(0, d_gain)
    mean_shift = by_image(d_shift * gain1) / count_two
    mean_gain = by_image(d_gain * gain1) / count_two
    back_gain1 = scaling1 * gain1
    back_mean1 = spread(-scaling1 * mean_shift, C2)
    back_normal1 = spread(scaling1 * mean_gain, C2)

    def unnorm(k, carry):
        rows = step_rows(k)
        for plane in range(4):
            normal = affine(x_ref[plane, rows], *normal1)
            back = affine(back_ref[plane, rows], back_gain1, back_mean1)
            back = back - scaled(normal, back_normal1)
            valid = inv_ref[plane, rows] > 0.0
            dx_ref[plane, rows] = jnp.where(valid, dx_ref[plane, rows] + back, 0.0)
        return carry

    sweep(unnorm, 0)

    def give_back(image, plane, line_place, there):
        image_ref[image, there] = dx_ref[plane, line_place]

    image_ref[...] = jnp.zeros(image_ref.shape, f32)
    each_image(size_ref, pair, give_back)

    def from_rows(within, carry):
        for spot in range(2 * STRIPS):
            image, strip = spot // STRIPS, spot % STRIPS
            start = pl.multiple_of((strip * SR + within) * LINE, LINE)
            target = strip_place(pair, spot, strip_count)
            payload_ref[target, within] = image_ref[image, pl.ds(start, CW)].astype(bf16)
        return carry

    lax.fori_loop(0, SR, from_rows, 0)

    def finish():
        copy = pltpu.make_async_copy(payload_ref, payload_hbm, sem)
        copy.start()
        vector_ref[...] = flat_ref[...]
        for n in range(3):
            vector_ref[n : n + 1] = jnp.sum(acc_ref[n], axis=0, keepdims=True)
        copy.wait()

    if pairs == 1:
        finish()
    else:
        pl.when(pair == pairs - 1)(finish)


def run_exit(sizes, state, back, flat, vec_two, strip_count):
    pairs = strip_count // 8
    payload = (strip_count, SR, CW, C2)
    make = pltpu.VMEM if pairs == 1 else jax.ShapeDtypeStruct
    plane_f32 = pltpu.VMEM((4, AREA, C2), f32)
    arrays = [*state, *back]
    if pairs == 1:
        arrays = held_in(pltpu.VMEM, *arrays)
    return pl.pallas_call(
        functools.partial(exit_kernel, pairs, strip_count),
        grid=() if pairs == 1 else (pairs,),
        in_specs=[SMEM]
        + pair_specs(pairs, STATE + BACK, pl.Buffered(1))
        + whole_specs(pairs, [flat.shape, vec_two.shape]),
        out_specs=[HBM] + whole_specs(pairs, [flat.shape]),
        out_shape=[pltpu.HBM(payload, bf16), make(flat.shape, f32)],
        scratch_shapes=[
            pltpu.VMEM(payload, bf16),
            pltpu.VMEM((2, CH * LINE, C2), f32),
            pltpu.VMEM((4, AREA + 2 * LINE, C2), f32),
            plane_f32,
            plane_f32,
            pltpu.VMEM((3, 8, C2), f32),
            pltpu.SemaphoreType.DMA,
        ],
        compiler_params=ROOMY,
        name="exit",
    )(sizes, *arrays, flat, vec_two)


def pack_kernel(master_ref, dense_ref):
    values = master_ref[...]
    dense_ref[...] = jnp.concatenate([values[:, :HALF], values[:, HALF:]], axis=2).astype(bf16)


def pack(master):
    owned = master.shape[0]
    return pl.pallas_call(
        pack_kernel,
        out_shape=jax.ShapeDtypeStruct((owned, HALF, 2 * BS), bf16),
        name="pack",
    )(master)


def fold_pair_kernel(near_ref, got_ref, own_ref, *part_refs):
    share = own_ref.shape[0]

    def one(n, carry):
        for k in range(len(part_refs) + 1):
            total = near_ref[k * share + n].astype(f32) + got_ref[k * share + n].astype(f32)
            if k == 0:
                own_ref[n] = total
            else:
                part_refs[k - 1][n] = total.astype(bf16)
        return carry

    lax.fori_loop(0, share, one, 0, unroll=4)


def fold_pair(near, got, groups):
    shape = ((near.shape[0] - 1) // groups,) + near.shape[1:]
    return pl.pallas_call(
        fold_pair_kernel,
        in_specs=[VMEM_BLOCK] * 2,
        out_specs=[VMEM_BLOCK] * groups,
        out_shape=[pltpu.VMEM(shape, f32)] + [pltpu.VMEM(shape, bf16)] * (groups - 1),
        compiler_params=ROOMY,
        name="fold_pair",
    )(*held_in(pltpu.VMEM, near, got))


def fold_tile_kernel(pieces, spot_ref, *refs):
    piece_refs, refs = refs[:pieces], refs[pieces:]
    vector_refs, refs = refs[:pieces], refs[pieces:]
    out_refs, sum_ref = refs[:-1], refs[-1]
    groups = len(out_refs)
    share = out_refs[0].shape[0]
    owned = piece_refs[0].shape[0]
    total = vector_refs[0][...]
    for ref in vector_refs[1:]:
        total = total + ref[...]
    for n in range(sum_ref.shape[0]):
        sum_ref[n] = jnp.zeros((HALF, 128), f32)
    for n in range(VEC_BLOCKS):
        sum_ref[n] = total[n * HALF : (n + 1) * HALF]

    def one(n, carry):
        for k, out_ref in enumerate(out_refs):
            number = lax.rem(spot_ref[0] + k, groups) * share + n
            block = jnp.minimum(number, owned - 1)
            total = piece_refs[0][block].astype(f32)
            for ref in piece_refs[1:]:
                total = total + ref[block].astype(f32)
            rest = sum_ref[jnp.maximum(number - owned, 0)]
            out_ref[n] = jnp.where(number < owned, total, rest).astype(out_ref.dtype)
        return carry

    lax.fori_loop(0, share, one, 0, unroll=share <= 16)


def fold_tile(spot, pieces, vectors, extra, groups):
    shape = ((pieces[0].shape[0] + extra) // groups,) + pieces[0].shape[1:]
    return pl.pallas_call(
        functools.partial(fold_tile_kernel, len(pieces)),
        in_specs=[SMEM] + [VMEM_BLOCK] * (len(pieces) + len(vectors)),
        out_specs=[VMEM_BLOCK] * groups,
        out_shape=[pltpu.VMEM(shape, f32)] + [pltpu.VMEM(shape, bf16)] * (groups - 1),
        scratch_shapes=[pltpu.VMEM((extra, HALF, 128), f32)],
        compiler_params=ROOMY,
        name="fold_tile",
    )(spot, *held_in(pltpu.VMEM, *pieces, *vectors))


def fold_batch_kernel(owned, vector_weight, spot_ref, *refs):
    part_refs, (total_ref, norm_ref) = refs[:-2], refs[-2:]
    share = total_ref.shape[0]
    square = jnp.zeros((8, 128), f32)
    for n in range(share):
        total = part_refs[0][n].astype(f32)
        for ref in part_refs[1:]:
            total = total + ref[n].astype(f32)
        total_ref[n] = total.astype(bf16)
        weight = jnp.where(spot_ref[0] * share + n < owned, 1.0, vector_weight)
        square = square + weight * fold(total * total)
    square = jnp.sum(jnp.sum(square, axis=1, keepdims=True), axis=0, keepdims=True)
    norm_ref[...] = jnp.broadcast_to(square[None], norm_ref.shape)


def fold_batch(spot, parts, owned, tile_count):
    count = tile_count * len(parts)
    return pl.pallas_call(
        functools.partial(fold_batch_kernel, owned, 1.0 / tile_count),
        in_specs=[SMEM] + [VMEM_BLOCK] * len(parts),
        out_specs=[VMEM_BLOCK] * 2,
        out_shape=[pltpu.VMEM(parts[0].shape, bf16), pltpu.VMEM((count, 1, 128), f32)],
        name="fold_batch",
    )(spot, *held_in(pltpu.VMEM, *parts))


def copies_between(sources, targets, sems, owned):
    return [
        [
            pltpu.make_async_copy(
                source.at[pl.ds(first, min(8, owned - first))],
                target.at[pl.ds(first, min(8, owned - first))],
                sems.at[len(sources) * n + k],
            )
            for k, (source, target) in enumerate(zip(sources, targets))
        ]
        for n, first in enumerate(range(0, owned, 8))
    ]


def groups_of(owned):
    return [(first, min(4, owned - first)) for first in range(0, owned, 4)]


def diagonal_of(count):
    order = (count * BS, count * BS)
    return lax.broadcasted_iota(jnp.int32, order, 0) // BS == (
        lax.broadcasted_iota(jnp.int32, order, 1) // BS
    )


def gather_kernel(owned, groups, spot_ref, *refs):
    quarters, refs = refs[:groups], refs[groups:]
    stat_hbm, stat_refs, refs = refs[:5], refs[5:10], refs[10:]
    grad_ref, left_ref, right_ref, vector_ref, in_sem = refs
    share = quarters[0].shape[0]
    copies = copies_between(stat_hbm, stat_refs, in_sem, owned)
    for arriving in copies:
        for copy in arriving:
            copy.start()
    left_half = lax.broadcasted_iota(jnp.int32, (HALF, 128), 1) < BS

    def summed(number):
        source = number // share
        local = number - source * share
        turn = lax.rem(spot_ref[0] - source + groups, groups)
        value = quarters[0][local].astype(f32)
        for k in range(1, groups):
            value = jnp.where(turn == k, quarters[k][local].astype(f32), value)
        return value

    for n in range(vector_ref.shape[0]):
        vector_ref[n] = summed(owned + n)
    for first, count in groups_of(owned):
        sides = []
        for n in range(first, first + count, 2):
            dense = summed(n)
            turned = pltpu.roll(dense, BS, 1)
            if n + 1 < first + count:
                second = summed(n + 1)
                top = jnp.where(left_half, dense, pltpu.roll(second, BS, 1))
                low = jnp.where(left_half, turned, second)
                side = jnp.concatenate([top, low], axis=0)
                grad_ref[n + 1] = pltpu.roll(side, BS, 1)[:, :BS]
            else:
                side = jnp.concatenate([dense, turned], axis=0)[:, :BS]
            grad_ref[n] = side[:, :BS]
            sides.append(side.astype(bf16))
        wide = jnp.concatenate(sides, axis=1)
        here = pl.ds(first, count)
        tall = jnp.where(diagonal_of(count), jnp.concatenate([wide] * count, axis=0), 0.0)
        left_ref[here] = product_nt(tall, wide).reshape(count, BS, BS)
        right = product_tn(wide, wide)
        for n in range(count):
            at = n // 2 * 128
            block = right[n * BS : n * BS + BS, at : min(at + 128, count * BS)]
            if n % 2:
                block = pltpu.roll(block, BS, 1)
            right_ref[first + n] = block[:, :BS]
    for arriving in copies:
        for copy in arriving:
            copy.wait()


def gather(spot, quarters, extra, *stats):
    shape = stats[0].shape
    groups = len(quarters)
    square = pltpu.VMEM(shape, f32)
    return pl.pallas_call(
        functools.partial(gather_kernel, shape[0], groups),
        in_specs=[SMEM] + [VMEM_BLOCK] * groups + [HBM] * 5,
        out_specs=[VMEM_BLOCK] * 9,
        out_shape=[square] * 8 + [pltpu.VMEM((extra, HALF, 128), f32)],
        scratch_shapes=[pltpu.SemaphoreType.DMA((5 * -(-shape[0] // 8),))],
        compiler_params=ROOMY,
        name="gather",
    )(spot, *held_in(pltpu.VMEM, *quarters), *held_in(pltpu.HBM, *stats))


def update_kernel(owned, *refs):
    norm_ref, stat_refs, (sum_ref, left_sum, right_sum, vector_sum) = refs[0], refs[1:6], refs[6:10]
    out_hbm, vector_ref, clip_ref, out_refs, out_sem = (
        refs[10:15],
        refs[15],
        refs[16],
        refs[17:22],
        refs[22],
    )
    master_ref, left_stat_ref, right_stat_ref, left_root_ref, right_root_ref = stat_refs
    grad_ref, left_ref, right_ref, new_ref, copy_ref = out_refs
    norm = jnp.sqrt(jnp.sum(norm_ref[...], axis=0))
    factor = jnp.minimum(1.0, clip_limit / norm)
    clip_ref[...] = norm
    vector_ref[...] = vector_sum[...] * factor
    factor = factor[:, :BS]
    copies = copies_between(out_refs, out_hbm, out_sem, owned)
    for first, count in groups_of(owned):
        here = pl.ds(first, count)
        grad = sum_ref[here] * factor
        grad_ref[here] = grad
        left_ref[here] = 0.5 * left_stat_ref[here] + left_sum[here] * factor * (0.5 * factor)
        right_ref[here] = 0.5 * right_stat_ref[here] + right_sum[here] * factor * (0.5 * factor)
        order = count * BS
        roots = left_root_ref[here].reshape(order, BS).astype(bf16)
        low = [grad[n].astype(bf16) for n in range(count)]
        wide = jnp.concatenate(low, axis=1)
        stepped = jnp.where(diagonal_of(count), product(roots, wide), 0.0).astype(bf16)
        roots = right_root_ref[here].reshape(order, BS).astype(bf16)
        stepped = product(stepped, roots).reshape(count, BS, BS)
        new = master_ref[here] - rate_matrix * stepped
        new_ref[here] = new
        copy_ref[here] = new.astype(bf16)
        if (first + count) % 8 == 0 or first + count == owned:
            for copy in copies[first // 8]:
                copy.start()
    for leaving in copies:
        for copy in leaving:
            copy.wait()


def update(norm, *arrays):
    shape = arrays[0].shape
    types = [f32] * 4 + [bf16]
    return pl.pallas_call(
        functools.partial(update_kernel, shape[0]),
        in_specs=[VMEM_BLOCK] * 10,
        out_specs=[HBM] * 5 + [VMEM_BLOCK] * 2,
        out_shape=[pltpu.HBM(shape, kind) for kind in types]
        + [
            jax.ShapeDtypeStruct(arrays[-1].shape, f32),
            jax.ShapeDtypeStruct((1, 128), f32),
        ],
        scratch_shapes=[pltpu.VMEM(shape, kind) for kind in types]
        + [pltpu.SemaphoreType.DMA((5 * -(-shape[0] // 8),))],
        compiler_params=ROOMY,
        name="update",
    )(*held_in(pltpu.VMEM, norm, *arrays))


def share_out(pieces, axis):
    return lax.all_to_all(pieces, axis, split_axis=0, concat_axis=0, tiled=True)


def swap(piece, distance):
    count = lax.axis_size("tile")
    return lax.ppermute(piece, "tile", [(i, i ^ distance) for i in range(count)])


def on_device(
    pixels,
    buckets,
    slot_owner_table,
    out_grad,
    master,
    left_stat,
    right_stat,
    left_root,
    right_root,
    vectors,
    moment,
):
    tile_count = lax.axis_size("tile")
    tile_place = lax.axis_index("tile")
    slot_count = pixels.shape[2]
    group_count = tile_count // STRIPS
    pairs = group_count // 2
    owned = master.shape[0]
    slots = owned * tile_count
    batch_count = lax.axis_size("batch")
    spot = lax.axis_index("batch").astype(jnp.int32).reshape(1)
    extra = extra_of(owned, batch_count)
    strips = share_out(pixels.reshape((tile_count,) + pixels.shape[3:]), "tile")
    dense = pack(master)
    paired = tile_count <= 8
    if paired:
        mine = [dense] + [swap(dense, 2 * k) for k in range(1, tile_count // 2)]
        pieces = mine + [swap(piece, 1) for piece in mine]
    else:
        pieces = [lax.all_gather(dense, "tile", axis=0, tiled=True)]

    numbers = jnp.arange(slots, dtype=jnp.int32)
    slot_of = jnp.sum(
        jnp.where(slot_owner_table[None, :] == numbers[:, None], numbers[None, :], 0), axis=1
    )
    owner = slot_of // owned
    within = slot_of - owner * owned
    place_of = slot_of
    if paired:
        apart = owner ^ tile_place
        apart = (apart & 1) * (tile_count // 2) + (apart >> 1)
        slot_of = place_of = within + owned * apart
    half = slots // 2
    near_place = jnp.where(place_of < half, place_of, half)
    far_place = jnp.where(place_of < half, half, place_of - half)
    image_ids = lax.dynamic_index_in_dim(
        buckets.reshape(group_count, slot_count), tile_place, 1, keepdims=False
    )
    turned = image_ids >= 2
    heights = jnp.where(image_ids == 0, 5 * CH // 9, jnp.where(image_ids == 1, 7 * CH // 9, CH))
    breadths = jnp.where(image_ids == 0, CW, jnp.where(image_ids == 1, 7 * CW // 9, 5 * CW // 9))
    sizes = jnp.stack(
        [
            jnp.where(turned, breadths, heights),
            jnp.where(turned, heights, breadths),
            turned,
        ],
        axis=1,
    )
    sizes = sizes.reshape(-1).astype(jnp.int32)

    two = 6 * C2 + HID2 + C2
    vec_two = jnp.concatenate([vectors[: 6 * C2], vectors[6 * C2 + HID2 : two]]).reshape(7, C2)
    vec_hid_two = vectors[6 * C2 : 6 * C2 + HID2].reshape(1, HID2)
    wide_end = two + 7 * C3
    vec_three = jnp.concatenate([vectors[two:wide_end], vectors[wide_end + HID3 :]])
    vec_three = jnp.pad(vec_three.reshape(8, C3), ((0, 0), (0, WIDE - C3)))
    vec_hid_three = vectors[wide_end : wide_end + HID3].reshape(1, HID3)

    flips = turned.reshape(-1, 1, 1, 1)
    goal = out_grad.reshape(2 * pairs, H3, W3, C3)
    goal = jnp.where(flips, goal.transpose(0, 2, 1, 3), goal)[:, :LINES]
    goal = goal.reshape(pairs, 2, LINES, W3, C3).transpose(0, 2, 3, 1, 4)
    goal = goal.reshape(pairs, LINES, 2 * W3, C3)
    goal = jnp.pad(goal, ((0, 0), (0, 0), (0, LINE - 2 * W3), (0, WIDE - C3)))
    goal = goal.reshape(pairs, AREA, WIDE)

    state = run_entry(sizes, strips, vec_two)
    result, *back, near, far, flat = run_main(
        (slot_of, near_place, far_place),
        sizes,
        state,
        goal,
        (vec_two, vec_hid_two, vec_three, vec_hid_three),
        pieces,
        tile_count,
    )
    pixel_back, vector = run_exit(sizes, state, back, flat, vec_two, tile_count)
    if paired:
        own, *parts = fold_pair(near, swap(far, 1), tile_count // 2)
        pieces = [own] + [swap(part, 2 * k + 2) for k, part in enumerate(parts)]
        vector, _ = lax.optimization_barrier((vector, parts[0]))
        vector = vector + swap(vector, 1)
        vectors_in = [vector] + [swap(vector, 2 * k) for k in range(1, tile_count // 2)]
    else:
        outgoing = jnp.concatenate([near[:half], far[:half]], axis=0)
        pieces = list(share_out(outgoing.reshape(tile_count, owned, HALF, 128), "tile"))
        vectors_in = list(lax.all_gather(vector, "tile"))
    result, pieces[1] = lax.optimization_barrier((result, pieces[1]))
    result = result.reshape(pairs, LINES, LINE, WIDE)[:, :, : 2 * W3, :C3]
    result = result.reshape(pairs, LINES, W3, 2, C3).transpose(0, 3, 1, 2, 4)
    result = result.reshape(2 * pairs, LINES, W3, C3)
    result = jnp.pad(result, ((0, 0), (0, H3 - LINES), (0, 0), (0, 0)))
    result = jnp.where(flips, result.transpose(0, 2, 1, 3), result)
    result = result.reshape(out_grad.shape)
    result, vectors_in[0] = lax.optimization_barrier((result, vectors_in[0]))
    own, *parts = fold_tile(spot, pieces, vectors_in, extra, batch_count)
    pixel_back, parts[0] = lax.optimization_barrier((pixel_back, parts[0]))
    returned = share_out(pixel_back, "tile").astype(f32).reshape(pixels.shape)
    parts = [
        lax.ppermute(part, "batch", [(i, (i + k + 1) % batch_count) for i in range(batch_count)])
        for k, part in enumerate(parts)
    ]
    quarter, norm = fold_batch(spot, [own] + parts, owned, tile_count)
    quarters = [quarter] + [
        lax.ppermute(quarter, "batch", [(i, (i + k) % batch_count) for i in range(batch_count)])
        for k in range(1, batch_count)
    ]
    norm = share_out(norm, ("batch", "tile"))
    gathered = gather(
        spot, quarters, extra, master, left_stat, right_stat, left_root, right_root
    )
    block_grad, left_new, right_new, master_new, weight_copy, whole_vector, clip = update(
        norm, *gathered
    )
    clip_norm = clip[0, 0]
    share = vectors.shape[0] // tile_count
    whole_vector = whole_vector.reshape(-1)
    vec_grad = lax.dynamic_slice_in_dim(whole_vector, tile_place * share, share, 0)
    vec_moment = moment + vec_grad * vec_grad
    own_vectors = lax.dynamic_slice_in_dim(vectors, tile_place * share, share, 0)
    vec_new = own_vectors - rate_vector * vec_grad / (jnp.sqrt(vec_moment) + eps_adagrad)
    return (
        result,
        returned,
        clip_norm,
        block_grad,
        left_new,
        right_new,
        master_new,
        weight_copy,
        vec_grad,
        vec_moment,
        vec_new,
    )


def solution(mesh):
    placed = (
        P("batch", "tile", None, None, None, None),
        P("batch"),
        P(),
        P("batch", "tile", None, None, None, None, None),
        P("tile", None, None),
        P("tile", None, None),
        P("tile", None, None),
        P("tile", None, None),
        P("tile", None, None),
        P(),
        P("tile"),
    )
    return jax.shard_map(
        on_device,
        mesh=mesh,
        in_specs=placed,
        out_specs=(
            P("batch", "tile", None, None, None, None, None),
            P("batch", "tile", None, None, None, None),
            P(),
            P("tile", None, None),
            P("tile", None, None),
            P("tile", None, None),
            P("tile", None, None),
            P("tile", None, None),
            P("tile"),
            P("tile"),
            P("tile"),
        ),
        check_vma=False,
    )
```

```python
import functools

import jax
import jax.numpy as jnp
from jax import lax
from jax.experimental import pallas as pl
from jax.experimental.pallas import tpu as pltpu
from jax.sharding import PartitionSpec as P

C2 = 128
HID2 = 512
C3 = 320
HID3 = 1280
CH = 36
CW = 36
STRIPS = 4
BS = 64
SR = CH // STRIPS
H3 = CH // 2
W3 = CW // 2
LONG = 7 * CH // 9
LINES = LONG // 2
WIDE = 384
LINE = 40
AREA = LINES * LINE
STEP = 2 * LINE
STEPS = AREA // STEP
HALF = BS // 2

eps_norm = 1e-05
clip_limit = 1.0
rate_matrix = 0.3
rate_vector = 0.3
eps_adagrad = 1e-08
f32 = jnp.float32
bf16 = jnp.bfloat16

SHAPES = [(C2, HID2), (HID2, C2), (9 * C2, C3), (C3, HID3), (HID3, C3)]
USED = sum(rows // BS * (cols // BS) for rows, cols in SHAPES)
VEC_ROWS = (6 * C2 + HID2 + C2 + C3 + 6 * C3 + HID3 + C3) // 128


VEC_BLOCKS = -(-VEC_ROWS // HALF)


def extra_of(owned, groups):
    return VEC_BLOCKS + -(owned + VEC_BLOCKS) % groups


def product(left, right):
    return jnp.dot(left, right, preferred_element_type=f32)


def product_nt(left, right):
    return lax.dot_general(left, right, (((1,), (1,)), ((), ())), preferred_element_type=f32)


def product_tn(left, right):
    return lax.dot_general(left, right, (((0,), (0,)), ((), ())), preferred_element_type=f32)


def gelu_pair(values):
    bell = jnp.exp2(values * values * (-0.5 * 1.4426950408889634))
    step = pl.reciprocal(1.0 + (0.3275911 * 0.7071067811865476) * jnp.abs(values), approx=True)
    tail = step * (
        0.5 * 0.254829592
        + step
        * (
            0.5 * -0.284496736
            + step
            * (0.5 * 1.421413741 + step * (0.5 * -1.453152027 + step * (0.5 * 1.061405429)))
        )
    )
    tail = tail * bell
    share = jnp.where(values >= 0.0, 1.0 - tail, tail)
    return (values * share, share + values * (bell * 0.3989422804014327))


def fold(values):
    chans = values.shape[-1]
    return jnp.sum(values.reshape(-1, 8, chans), axis=0)


def by_image(total):
    total = total + pltpu.roll(total, 4, 0)
    total = total + pltpu.roll(total, 2, 0)
    return jnp.sum(total, axis=1, keepdims=True)


def line(pattern):
    return jnp.concatenate([pattern] * (LINE // 8), axis=0)


def spread(pattern, chans):
    return jnp.broadcast_to(pattern, (8, chans))


def affine(values, factor, shift):
    tiles = values.reshape(-1, 8, values.shape[-1])
    return (tiles * factor + shift).reshape(values.shape)


def scaled(values, factor):
    tiles = values.reshape(-1, 8, values.shape[-1])
    return (tiles * factor).reshape(values.shape)


def from_left(values):
    return pltpu.roll(values, 2, 0)


def from_right(values):
    return pltpu.roll(values, values.shape[0] - 2, 0)


def rounded(values):
    return values.astype(bf16).astype(f32)


def widen(values):
    return jnp.concatenate([values] * (WIDE // 128), axis=-1)


def norm_terms(total, square, count):
    mean = by_image(total) / count
    scaling = lax.rsqrt(by_image(square) / count - mean * mean + eps_norm)
    return (mean, scaling)


def sweep(visit, start):
    return lax.fori_loop(0, STEPS, visit, start, unroll=True)


def step_rows(k, lines=0):
    start = k * STEP + lines * LINE
    return pl.ds(start if isinstance(k, int) else pl.multiple_of(start, LINE), STEP)


def held_in(space, *arrays):
    return [pltpu.with_memory_space_constraint(array, space) for array in arrays]


VMEM_BLOCK = pl.BlockSpec(memory_space=pltpu.VMEM)
HBM = pl.BlockSpec(memory_space=pltpu.HBM)
SMEM = pl.BlockSpec(memory_space=pltpu.SMEM)


def roomy(mebibytes):
    return pltpu.CompilerParams(vmem_limit_bytes=mebibytes * 1024 * 1024)


class Geometry:
    def __init__(self, size_ref, pair):
        parity = lax.broadcasted_iota(jnp.int32, (8, 128), 0) % 2
        high, broad, turned = (
            jnp.where(parity == 0, size_ref[pair * 6 + n], size_ref[pair * 6 + 3 + n])
            for n in range(3)
        )
        self.high = high
        self.count_two = (high * broad * C2).astype(f32)[:, :1]
        self.high3 = (high + 1) // 2
        broad3 = (broad + 1) // 2
        self.count_three = (self.high3 * broad3 * C3).astype(f32)[:, :1]
        place = lax.broadcasted_iota(jnp.int32, (LINE, 128), 0) // 2
        inside = lax.broadcasted_iota(jnp.int32, (LINE, 128), 0) < 2 * W3
        self.reach = []
        self.col_share = []
        for pc in range(2):
            column = 2 * place + pc
            self.reach.append(jnp.where(inside & (column < line(broad)), line(high), 0))
            edge = (column == 0) | (column == line(broad) - 1)
            self.col_share.append(jnp.where(edge, 0.5, 1.0 / 3.0))
        self.reach3 = jnp.where(inside & (place < line(broad3)), line(self.high3), 0)
        edge3 = (place == 0) | (place == line(broad3) - 1)
        self.col_share3 = jnp.where(edge3, 0.5, 1.0 / 3.0)
        self.flipped = jnp.concatenate([turned] * (STEP // 8), axis=0) > 0

    def share(self, plane, k):
        pr, pc = plane // 2, plane % 2
        return self.lines(4 * k + pr, 2, self.reach[pc], self.col_share[pc], self.high)

    def share3(self, k):
        return self.lines(2 * k, 1, self.reach3, self.col_share3, self.high3)

    def lines(self, row, stride, reach, col_share, height):
        parts = []
        for n in range(2):
            here = row + stride * n
            row_share = jnp.where((here == 0) | (here == height - 1), 0.5, 1.0 / 3.0)
            parts.append(jnp.where(here < reach, line(row_share) * col_share, 0.0))
        return jnp.concatenate(parts, axis=0)


def strip_place(pair, spot, strip_count):
    return lax.rem(pair * 8 + strip_count - 2 + spot, strip_count)


def each_image(size_ref, pair, visit):
    for image in range(2):
        way = size_ref[pair * 6 + 3 * image + 2]
        for flat in (True, False):

            @pl.when(way == (0 if flat else 1))
            def _():
                def one(r, carry):
                    for pr in range(2):
                        for pc in range(2):
                            line_place = pl.ds(r * LINE + image, W3, stride=2)
                            if flat:
                                there = pl.ds((2 * r + pr) * LINE + pc, W3, stride=2)
                            else:
                                there = pl.ds(pc * LINE + 2 * r + pr, W3, stride=2 * LINE)
                            visit(image, pr * 2 + pc, line_place, there)
                    return carry

                lax.fori_loop(0, LINES, one, 0)


def row_windows(col_ref, pc, k):
    both = col_ref[pc, step_rows(k, 1)] + col_ref[2 + pc, step_rows(k, 1)]
    return (both + col_ref[2 + pc, step_rows(k)], both + col_ref[pc, step_rows(k, 2)])


def put_col_windows(col_ref, pr, k, even, odd):
    both = even + odd
    col_ref[pr * 2, step_rows(k, 1)] = both + from_left(odd)
    col_ref[pr * 2 + 1, step_rows(k, 1)] = both + from_right(even)


def clear_edges(col_ref):
    zero_line = jnp.zeros((LINE, C2), f32)
    for plane in range(4):
        col_ref[plane, 0:LINE] = zero_line
        col_ref[plane, AREA + LINE : AREA + 2 * LINE] = zero_line


def entry_kernel(
    pairs,
    strip_count,
    size_ref,
    strips_ref,
    vec_two_ref,
    x_out,
    inv_out,
    pool_out,
    mix_out,
    stat_out,
    image_ref,
    col_ref,
):
    pair = pl.program_id(0) if pairs > 1 else 0
    x_ref, inv_ref, pool_ref, mix_ref = (ref.at[0] for ref in (x_out, inv_out, pool_out, mix_out))
    shape = Geometry(size_ref, pair)
    gain1, bias1, scale1 = (vec_two_ref[n : n + 1] for n in range(3))
    clear_edges(col_ref)

    def to_rows(within, carry):
        for spot in range(2 * STRIPS):
            image, strip = spot // STRIPS, spot % STRIPS
            start = pl.multiple_of((strip * SR + within) * LINE, LINE)
            source = strip_place(pair, spot, strip_count)
            image_ref[image, pl.ds(start, CW)] = strips_ref[source, within].astype(f32)
        return carry

    lax.fori_loop(0, SR, to_rows, 0)

    def take_in(image, plane, line_place, there):
        x_ref[plane, line_place] = image_ref[image, there]

    each_image(size_ref, pair, take_in)

    def arrange(k, carry):
        total, square = carry
        rows = step_rows(k)
        for plane in range(4):
            share = shape.share(plane, k)
            inv_ref[plane, rows] = share
            values = jnp.where(share > 0.0, x_ref[plane, rows], 0.0)
            x_ref[plane, rows] = values
            total = total + fold(values)
            square = square + fold(values * values)
        return (total, square)

    nothing = jnp.zeros((8, C2), f32)
    total, square = sweep(arrange, (nothing, nothing))
    mean1, scaling1 = norm_terms(total, square, shape.count_two)
    factor1 = scaling1 * gain1
    shift1 = bias1 - mean1 * scaling1 * gain1

    def window_cols(k, carry):
        rows = step_rows(k)
        for pr in range(2):
            masked = []
            for pc in range(2):
                plane = pr * 2 + pc
                normal = rounded(affine(x_ref[plane, rows], factor1, shift1))
                masked.append(jnp.where(inv_ref[plane, rows] > 0.0, normal, 0.0))
            put_col_windows(col_ref, pr, k, *masked)
        return carry

    sweep(window_cols, 0)

    def mix(k, carry):
        total, square = carry
        rows = step_rows(k)
        for pc in range(2):
            windows = row_windows(col_ref, pc, k)
            for pr in range(2):
                plane = pr * 2 + pc
                values = x_ref[plane, rows]
                share = inv_ref[plane, rows]
                pooled = windows[pr] * share - rounded(affine(values, factor1, shift1))
                pooled = jnp.where(share > 0.0, pooled, 0.0)
                mixed = values + scale1 * pooled
                pool_ref[plane, rows] = pooled
                mix_ref[plane, rows] = mixed
                total = total + fold(mixed)
                square = square + fold(mixed * mixed)
        return (total, square)

    total, square = sweep(mix, (nothing, nothing))
    mean2, scaling2 = norm_terms(total, square, shape.count_two)
    for n, value in enumerate((mean1, scaling1, mean2, scaling2)):
        stat_out[0, n] = spread(value, 128)


def pair_specs(pairs, shapes, mode=None):
    if pairs == 1:
        return [VMEM_BLOCK] * len(shapes)
    return [
        pl.BlockSpec(
            (1,) + shape, lambda t, rank=len(shape): (t,) + (0,) * rank, pipeline_mode=mode
        )
        for shape in shapes
    ]


def whole_specs(pairs, shapes):
    if pairs == 1:
        return [VMEM_BLOCK] * len(shapes)
    return [
        pl.BlockSpec(
            shape,
            lambda t, rank=len(shape): (0,) * rank,
            pipeline_mode=pl.Buffered(1),
        )
        for shape in shapes
    ]


def pair_arrays(pairs, shapes, kinds):
    make = pltpu.VMEM if pairs == 1 else jax.ShapeDtypeStruct
    return [make((pairs,) + shape, kind) for shape, kind in zip(shapes, kinds)]


STATE = [(4, AREA, C2)] * 4 + [(4, 8, 128)]
BACK = [(4, AREA, C2)] * 2 + [(2, 8, 128)]


def run_entry(sizes, strips, vec_two):
    strip_count = strips.shape[0]
    pairs = strip_count // 8
    return pl.pallas_call(
        functools.partial(entry_kernel, pairs, strip_count),
        grid=() if pairs == 1 else (pairs,),
        in_specs=[SMEM] + whole_specs(pairs, [strips.shape, vec_two.shape]),
        out_specs=pair_specs(pairs, STATE),
        out_shape=pair_arrays(pairs, STATE, [f32] * 5),
        scratch_shapes=[
            pltpu.VMEM((2, CH * LINE, C2), f32),
            pltpu.VMEM((4, AREA + 2 * LINE, C2), f32),
        ],
        compiler_params=roomy(6 if pairs == 1 else 40),
        name="entry",
    )(sizes, strips, vec_two)


WEIGHTS = [(C2, HID2), (HID2, C2), (9 * C2, WIDE), (WIDE, HID3), (HID3, WIDE)]


def unpack_kernel(piece_count, slot_ref, *refs):
    piece_refs, refs = refs[:piece_count], refs[piece_count:]
    weights, gathered_ref = refs[:-1], refs[-1]
    count = piece_refs[0].shape[0]
    for n, ref in enumerate(piece_refs):
        gathered_ref[n * count : n * count + count] = ref[...]
    left_half = lax.broadcasted_iota(jnp.int32, (HALF, 128), 1) < BS
    offset = 0
    for (rows, cols), ref in zip(SHAPES, weights):
        wide = cols // BS
        for rb in range(rows // BS):
            for cb in range(0, wide, 2):
                number = offset + rb * wide + cb
                first = gathered_ref[slot_ref[number]]
                turned = pltpu.roll(first, BS, 1)
                if cb + 1 < wide:
                    second = gathered_ref[slot_ref[number + 1]]
                    top = jnp.where(left_half, first, pltpu.roll(second, BS, 1))
                    low = jnp.where(left_half, turned, second)
                else:
                    top = jnp.where(left_half, first, 0.0)
                    low = jnp.where(left_half, turned, 0.0)
                place = slice(cb * BS, cb * BS + 128)
                ref[rb * BS : rb * BS + HALF, place] = top
                ref[rb * BS + HALF : rb * BS + BS, place] = low
        offset += rows // BS * wide
    weights[3][C3:, :] = jnp.zeros((WIDE - C3, HID3), bf16)


def run_unpack(slot_of, pieces):
    slots = sum(piece.shape[0] for piece in pieces)
    return pl.pallas_call(
        functools.partial(unpack_kernel, len(pieces)),
        in_specs=[SMEM] + [VMEM_BLOCK] * len(pieces),
        out_specs=[VMEM_BLOCK] * 5,
        out_shape=[pltpu.VMEM(shape, bf16) for shape in WEIGHTS],
        scratch_shapes=[pltpu.VMEM((slots, HALF, 128), bf16)],
        compiler_params=roomy(6),
        name="unpack",
    )(slot_of, *held_in(pltpu.VMEM, *pieces))


def main_kernel(
    pairs,
    strip_count,
    slots,
    near_place,
    far_place,
    size_ref,
    inv_in,
    mix_in,
    stat_in,
    goal_ref,
    vec_two_ref,
    vec_hid_two_ref,
    vec_three_ref,
    vec_hid_three_ref,
    w1_ref,
    w2_ref,
    we_ref,
    w3_ref,
    w4_ref,
    result_ref,
    zed_out,
    dx_out,
    mean_out,
    near_ref,
    far_ref,
    flat_ref,
    zed_ref,
    hid_ref,
    u_ref,
    g_ref,
    h_ref,
    dy_ref,
    patch_ref,
    dpatch_ref,
    inv3_ref,
    e_ref,
    col3_ref,
    pool3_ref,
    mix3_ref,
    dx3_ref,
    hid3_ref,
    dhid3_ref,
    u3_ref,
    g3_ref,
    h3_ref,
    dy3_ref,
    dpre_ref,
    gw1_ref,
    gw2_ref,
    gwe_ref,
    gw3_ref,
    gw4_ref,
    acc_two,
    acc_hid_two,
    acc_three,
    acc_hid_three,
):
    pair = pl.program_id(0) if pairs > 1 else 0
    grads = [gw1_ref, gw2_ref, gwe_ref, gw3_ref, gw4_ref]
    inv_ref, mix_ref, stat_ref = (ref.at[0] for ref in (inv_in, mix_in, stat_in))
    back_ref, dx_ref = zed_out.at[0], dx_out.at[0]
    left_half = lax.broadcasted_iota(jnp.int32, (HALF, 128), 1) < BS

    def at_pair(number, act):
        if pairs == 1:
            act()
        else:
            pl.when(pair == number)(act)

    def begin():
        acc_two[...] = jnp.zeros(acc_two.shape, f32)
        acc_hid_two[...] = jnp.zeros(acc_hid_two.shape, f32)
        acc_three[...] = jnp.zeros(acc_three.shape, f32)
        acc_hid_three[...] = jnp.zeros(acc_hid_three.shape, f32)

    at_pair(0, begin)
    shape = Geometry(size_ref, pair)
    count_two, count_three, flipped = shape.count_two, shape.count_three, shape.flipped
    nothing = jnp.zeros((8, C2), f32)
    nothing3 = jnp.zeros((8, WIDE), f32)
    gain2, bias2, scale2, out_bias = (vec_two_ref[n : n + 1] for n in range(3, 7))
    embed_bias, gain3, bias3, scale3 = (vec_three_ref[n : n + 1] for n in range(4))
    gain4, bias4, scale4, out_bias3 = (vec_three_ref[n : n + 1] for n in range(4, 8))
    mean2, scaling2 = stat_ref[2], stat_ref[3]
    factor2 = scaling2 * gain2
    shift2 = bias2 - mean2 * scaling2 * gain2
    for plane in range(4):
        zed_ref[plane, 0:LINE] = jnp.zeros((LINE, C2), f32)
    col3_ref[0:LINE] = jnp.zeros((LINE, WIDE), f32)
    col3_ref[AREA + LINE : AREA + 2 * LINE] = jnp.zeros((LINE, WIDE), f32)

    def put_block(number, block):
        near_ref[near_place[number]] = block
        far_ref[far_place[number]] = block

    def pack_blocks(matrices):
        offsets = [0]
        for rows, cols in SHAPES:
            offsets.append(offsets[-1] + rows // BS * (cols // BS))
        for which in matrices:
            (rows, cols), ref = SHAPES[which], grads[which]
            wide = cols // BS
            for rb in range(rows // BS):
                for cb in range(0, wide, 2):
                    number = offsets[which] + rb * wide + cb
                    at = slice(cb * BS, cb * BS + 128)
                    top = ref[rb * BS : rb * BS + HALF, at].astype(bf16)
                    low = ref[rb * BS + HALF : rb * BS + BS, at].astype(bf16)
                    put_block(number, jnp.where(left_half, top, pltpu.roll(low, BS, 1)))
                    if cb + 1 < wide:
                        put_block(number + 1, jnp.where(left_half, pltpu.roll(top, BS, 1), low))

    def plane_rows(plane):
        return slice(plane * AREA, plane * AREA + AREA)

    def begin_plane(plane):
        low = affine(mix_ref[plane], factor2, shift2).astype(bf16)
        h_ref[plane_rows(plane)] = low
        hid_ref[plane % 2] = product(low, w1_ref[...])

    begin_plane(0)
    for plane in range(4):
        if plane < 3:
            begin_plane(plane + 1)
        for k in range(STEPS):
            rows = step_rows(k)
            flat = slice(plane * AREA + k * STEP, plane * AREA + k * STEP + STEP)
            for at in range(0, HID2, 128):
                lanes = slice(at, at + 128)
                active, slope = gelu_pair(hid_ref[plane % 2, rows, lanes] + vec_hid_two_ref[:, lanes])
                u_ref[flat, lanes] = active.astype(bf16)
                g_ref[flat, lanes] = slope.astype(bf16)
        out = product(u_ref[plane_rows(plane)], w2_ref[...]) + out_bias
        zed = jnp.where(inv_ref[plane] > 0.0, mix_ref[plane] + scale2 * out, 0.0)
        zed_ref[plane, LINE : LINE + AREA] = rounded(zed)

    def patches(k, carry):
        rows = step_rows(k)
        taps = []
        for ky in range(3):
            pr = (0 if ky == 1 else 1) * 2
            source = step_rows(k, 0 if ky == 0 else 1)
            even = zed_ref[pr, source]
            odd = zed_ref[pr + 1, source]
            taps.append((from_left(odd), even, odd))
        for ky in range(3):
            for kx in range(3):
                at = (3 * ky + kx) * C2
                tap = taps[ky][kx]
                if ky != kx:
                    tap = jnp.where(flipped, taps[kx][ky], tap)
                patch_ref[rows, at : at + C2] = tap.astype(bf16)
        return carry

    sweep(patches, 0)
    e_ref[...] = product(patch_ref[...], we_ref[...])

    def embed(k, carry):
        total, square = carry
        rows = step_rows(k)
        share = shape.share3(k)
        inv3_ref[rows] = share
        out = jnp.where(widen(share) > 0.0, e_ref[rows] + embed_bias, 0.0)
        e_ref[rows] = out
        return (total + fold(out), square + fold(out * out))

    total, square = sweep(embed, (nothing3, nothing3))
    mean3, scaling3 = norm_terms(total, square, count_three)
    factor3 = scaling3 * gain3
    shift3 = bias3 - mean3 * scaling3 * gain3

    def window_cols3(k, carry):
        rows = step_rows(k)
        normal = rounded(affine(e_ref[rows], factor3, shift3))
        masked = jnp.where(widen(inv3_ref[rows]) > 0.0, normal, 0.0)
        col3_ref[step_rows(k, 1)] = masked + from_left(masked) + from_right(masked)
        return carry

    sweep(window_cols3, 0)

    def row_windows3(k):
        return col3_ref[step_rows(k)] + col3_ref[step_rows(k, 1)] + col3_ref[step_rows(k, 2)]

    def mix3(k, carry):
        total, square = carry
        rows = step_rows(k)
        values = e_ref[rows]
        share = widen(inv3_ref[rows])
        pooled = row_windows3(k) * share - rounded(affine(values, factor3, shift3))
        pooled = jnp.where(share > 0.0, pooled, 0.0)
        mixed = values + scale3 * pooled
        pool3_ref[rows] = pooled
        mix3_ref[rows] = mixed
        return (total + fold(mixed), square + fold(mixed * mixed))

    total, square = sweep(mix3, (nothing3, nothing3))
    mean4, scaling4 = norm_terms(total, square, count_three)
    factor4 = scaling4 * gain4
    shift4 = bias4 - mean4 * scaling4 * gain4
    normal4 = (spread(scaling4, WIDE), spread(-mean4 * scaling4, WIDE))

    def prepare3(k, d_bias):
        rows = step_rows(k)
        h3_ref[rows] = affine(mix3_ref[rows], factor4, shift4).astype(bf16)
        goal = goal_ref[0, rows].astype(f32)
        goal = jnp.where(widen(inv3_ref[rows]) > 0.0, goal, 0.0)
        low_goal = (scale4 * goal).astype(bf16)
        dy3_ref[rows] = low_goal
        return d_bias + fold(low_goal.astype(f32))

    acc_three[7] += sweep(prepare3, nothing3)

    def keep(ref, value, place=slice(None)):
        if pairs == 1:
            ref[place] = value.astype(ref.dtype)
        else:

            @pl.when(pair == 0)
            def _():
                ref[place] = value

            @pl.when(pair > 0)
            def _():
                ref[place] += value

    def begin_chunk(at):
        lanes = slice(at, at + 256)
        hid3_ref[:, lanes] = product(h3_ref[...], w3_ref[:, lanes])
        dhid3_ref[:, lanes] = product_nt(dy3_ref[...], w4_ref[lanes])

    begin_chunk(0)
    for at in range(0, HID3, 256):
        if at + 256 < HID3:
            begin_chunk(at + 256)
        for lane in (at, at + 128):
            lanes = slice(lane, lane + 128)
            total = nothing
            for k in range(STEPS):
                rows = step_rows(k)
                active, slope = gelu_pair(hid3_ref[rows, lanes] + vec_hid_three_ref[:, lanes])
                u3_ref[rows, lanes] = active.astype(bf16)
                low = (slope * dhid3_ref[rows, lanes]).astype(bf16)
                g3_ref[rows, lanes] = low
                total = total + fold(low.astype(f32))
            acc_hid_three[:, lanes] += total
        lanes = slice(at, at + 256)
        out = product(u3_ref[:, lanes], w4_ref[lanes])
        d_low = product_nt(g3_ref[:, lanes], w3_ref[:, lanes])
        result_ref[0] = out if at == 0 else result_ref[0] + out
        dx3_ref[...] = d_low if at == 0 else dx3_ref[...] + d_low
        keep(gw3_ref, product_tn(h3_ref[...], g3_ref[:, lanes]), (slice(None), lanes))
        keep(gw4_ref, product_tn(u3_ref[:, lanes], dy3_ref[...]), lanes)

    def finish3(k, carry):
        d_scale, d_shift, d_gain = carry
        rows = step_rows(k)
        valid = widen(inv3_ref[rows]) > 0.0
        mixed = mix3_ref[rows]
        out = jnp.where(valid, result_ref[0, rows] + out_bias3, 0.0)
        result_ref[0, rows] = mixed + scale4 * out
        d_scale = d_scale + fold(out * goal_ref[0, rows].astype(f32))
        d_low = dx3_ref[rows]
        normal = affine(mixed, *normal4)
        return (d_scale, d_shift + fold(d_low), d_gain + fold(d_low * normal))

    d_scale, d_shift, d_gain = sweep(finish3, (nothing3, nothing3, nothing3))
    acc_three[6] += d_scale
    acc_three[5] += d_shift
    acc_three[4] += d_gain
    mean_shift = by_image(d_shift * gain4) / count_three
    mean_gain = by_image(d_gain * gain4) / count_three
    back_gain4 = scaling4 * gain4
    back_mean4 = spread(-scaling4 * mean_shift, WIDE)
    back_normal4 = spread(scaling4 * mean_gain, WIDE)

    def unmix3(k, d_scale):
        rows = step_rows(k)
        share = widen(inv3_ref[rows])
        valid = share > 0.0
        normal = affine(mix3_ref[rows], *normal4)
        back = affine(dx3_ref[rows], back_gain4, back_mean4) - scaled(normal, back_normal4)
        d_mixed = jnp.where(valid, back + goal_ref[0, rows].astype(f32), 0.0)
        dx3_ref[rows] = d_mixed
        d_scale = d_scale + fold(pool3_ref[rows] * d_mixed)
        weighted = scale3 * d_mixed * share
        col3_ref[step_rows(k, 1)] = weighted + from_left(weighted) + from_right(weighted)
        return d_scale

    acc_three[3] += sweep(unmix3, nothing3)
    normal3 = (spread(scaling3, WIDE), spread(-mean3 * scaling3, WIDE))

    def unpool3(k, carry):
        d_shift, d_gain = carry
        rows = step_rows(k)
        valid = widen(inv3_ref[rows]) > 0.0
        d_normal = jnp.where(valid, row_windows3(k) - scale3 * dx3_ref[rows], 0.0)
        pool3_ref[rows] = d_normal
        normal = affine(e_ref[rows], *normal3)
        return (d_shift + fold(d_normal), d_gain + fold(d_normal * normal))

    d_shift, d_gain = sweep(unpool3, (nothing3, nothing3))
    acc_three[2] += d_shift
    acc_three[1] += d_gain
    mean_shift = by_image(d_shift * gain3) / count_three
    mean_gain = by_image(d_gain * gain3) / count_three
    back_gain3 = scaling3 * gain3
    back_mean3 = spread(-scaling3 * mean_shift, WIDE)
    back_normal3 = spread(scaling3 * mean_gain, WIDE)

    def unnorm3(k, d_bias):
        rows = step_rows(k)
        valid = widen(inv3_ref[rows]) > 0.0
        normal = affine(e_ref[rows], *normal3)
        back = affine(pool3_ref[rows], back_gain3, back_mean3) - scaled(normal, back_normal3)
        low = jnp.where(valid, dx3_ref[rows] + back, 0.0).astype(bf16)
        dpre_ref[rows] = low
        return d_bias + fold(low.astype(f32))

    acc_three[0] += sweep(unnorm3, nothing3)
    keep(gwe_ref, product_tn(patch_ref[...], dpre_ref[...]))
    dpatch_ref[0:AREA] = product_nt(dpre_ref[...], we_ref[...])
    dpatch_ref[AREA : AREA + LINE] = jnp.zeros((LINE, 9 * C2), f32)

    def gather_back(k, carry):
        rows = step_rows(k)

        def tap(ky, kx, source):
            at = (3 * ky + kx) * C2
            value = dpatch_ref[source, at : at + C2]
            if ky != kx:
                at = (3 * kx + ky) * C2
                value = jnp.where(flipped, dpatch_ref[source, at : at + C2], value)
            return value

        sources = []
        for ky in range(3):
            source = step_rows(k, 1 if ky == 0 else 0)
            sources.append(
                (tap(ky, 1, source), tap(ky, 2, source) + from_right(tap(ky, 0, source)))
            )
        for pc in range(2):
            for pr, value in ((0, sources[1][pc]), (1, sources[2][pc] + sources[0][pc])):
                plane = pr * 2 + pc
                valid = inv_ref[plane, rows] > 0.0
                back_ref[plane, rows] = jnp.where(valid, rounded(value), 0.0)
        return carry

    sweep(gather_back, 0)

    if pairs == 1:
        pack_blocks(range(2, 5))

    normal2 = (spread(scaling2, C2), spread(-mean2 * scaling2, C2))

    def begin_back(plane):
        low_goal = (scale2 * back_ref[plane]).astype(bf16)
        dy_ref[plane_rows(plane)] = low_goal
        hid_ref[plane % 2] = product_nt(low_goal, w2_ref[...])
        return fold(low_goal.astype(f32))

    d_out_bias = begin_back(0)
    d_shift, d_gain = nothing, nothing
    sums = [nothing] * (HID2 // 128)
    new_gw1, new_gw2 = None, None
    for plane in range(4):
        if plane < 3:
            d_out_bias = d_out_bias + begin_back(plane + 1)
        for k in range(STEPS):
            rows = step_rows(k)
            part = slice(plane * AREA + k * STEP, plane * AREA + k * STEP + STEP)
            for n, at in enumerate(range(0, HID2, 128)):
                lanes = slice(at, at + 128)
                low = g_ref[part, lanes].astype(f32) * hid_ref[plane % 2, rows, lanes]
                low = low.astype(bf16)
                g_ref[part, lanes] = low
                sums[n] = sums[n] + fold(low.astype(f32))
        flat = plane_rows(plane)
        d_low = product_nt(g_ref[flat], w1_ref[...])
        dx_ref[plane] = d_low
        d_shift = d_shift + fold(d_low)
        d_gain = d_gain + fold(d_low * affine(mix_ref[plane], *normal2))
        part_gw1 = product_tn(h_ref[flat], g_ref[flat])
        part_gw2 = product_tn(dy_ref[flat], u_ref[flat])
        new_gw1 = part_gw1 if plane == 0 else new_gw1 + part_gw1
        new_gw2 = part_gw2 if plane == 0 else new_gw2 + part_gw2
    new_gw2 = new_gw2.T
    for n, value in enumerate(sums):
        acc_hid_two[:, n * 128 : n * 128 + 128] += value
    acc_two[6] += d_out_bias
    acc_two[4] += d_shift
    acc_two[3] += d_gain
    mean_out[0, 0] = spread(by_image(d_shift * gain2) / count_two, 128)
    mean_out[0, 1] = spread(by_image(d_gain * gain2) / count_two, 128)
    keep(gw1_ref, new_gw1)
    keep(gw2_ref, new_gw2)
    d_scale = fold(w2_ref[...].astype(f32) * new_gw2) + out_bias * d_out_bias
    acc_two[5] += d_scale / scale2

    def finish():
        if pairs > 1:
            pack_blocks(range(5))
        else:
            pack_blocks(range(2))

        def filler(number, carry):
            put_block(number, jnp.zeros((HALF, 128), bf16))
            return carry

        lax.fori_loop(USED, slots, filler, 0)

        flat_ref[...] = jnp.zeros(flat_ref.shape, f32)

        def put(at, total, length):
            if at % 128:
                room = jnp.zeros((8, 128), f32)
                if total.shape[1] < length + BS:
                    total = jnp.concatenate([total, room], axis=1)
                total = pltpu.roll(total, BS, 1)
            whole = jnp.sum(total, axis=0, keepdims=True)
            done = -(at % 128)
            row = at // 128
            lane = 0
            while done < length:
                first = max(0, -done)
                last = min(128, length - done)
                flat_ref[row : row + 1, first:last] = whole[:, lane + first : lane + last]
                done += 128
                lane += 128
                row += 1

        at = 3 * C2
        for n in range(3, 6):
            put(at, acc_two[n], C2)
            at += C2
        put(at, acc_hid_two[...], HID2)
        at += HID2
        put(at, acc_two[6], C2)
        at += C2
        for n in range(7):
            put(at, acc_three[n], C3)
            at += C3
        put(at, acc_hid_three[...], HID3)
        at += HID3
        put(at, acc_three[7], C3)

    at_pair(pairs - 1, finish)


def run_main(places, sizes, state, goal, vectors, weights, strip_count):
    pairs = goal.shape[0]
    slots = places[0].shape[0]
    half = slots // 2 + 1
    if pairs == 1:
        state = held_in(pltpu.VMEM, *state)
    weights = held_in(pltpu.VMEM, *weights)
    _, inv, _, mix, stat = state
    state_shapes = [STATE[1], STATE[3], STATE[4]]
    grad_kind = bf16 if pairs == 1 else f32
    wide_f32 = pltpu.VMEM((AREA, WIDE), f32)
    wide_bf16 = pltpu.VMEM((AREA, WIDE), bf16)
    scratch = [
        pltpu.VMEM((4, AREA + LINE, C2), f32),
        pltpu.VMEM((2, AREA, HID2), f32),
        pltpu.VMEM((4 * AREA, HID2), bf16),
        pltpu.VMEM((4 * AREA, HID2), bf16),
        pltpu.VMEM((4 * AREA, C2), bf16),
        pltpu.VMEM((4 * AREA, C2), bf16),
        pltpu.VMEM((AREA, 9 * C2), bf16),
        pltpu.VMEM((AREA + LINE, 9 * C2), f32),
        pltpu.VMEM((AREA, 128), f32),
        wide_f32,
        pltpu.VMEM((AREA + 2 * LINE, WIDE), f32),
        wide_f32,
        wide_f32,
        wide_f32,
        pltpu.VMEM((AREA, HID3), f32),
        pltpu.VMEM((AREA, HID3), f32),
        pltpu.VMEM((AREA, HID3), bf16),
        pltpu.VMEM((AREA, HID3), bf16),
        wide_bf16,
        wide_bf16,
        wide_bf16,
        pltpu.VMEM((C2, HID2), grad_kind),
        pltpu.VMEM((HID2, C2), grad_kind),
        pltpu.VMEM((9 * C2, WIDE), grad_kind),
        pltpu.VMEM((WIDE, HID3), grad_kind),
        pltpu.VMEM((HID3, WIDE), grad_kind),
        pltpu.VMEM((7, 8, C2), f32),
        pltpu.VMEM((8, HID2), f32),
        pltpu.VMEM((8, 8, WIDE), f32),
        pltpu.VMEM((8, HID3), f32),
    ]
    out_shapes = [(half, HALF, 128), (half, HALF, 128), (VEC_BLOCKS * HALF, 128)]
    make = pltpu.VMEM if pairs == 1 else jax.ShapeDtypeStruct
    return pl.pallas_call(
        functools.partial(main_kernel, pairs, strip_count, slots),
        grid=() if pairs == 1 else (pairs,),
        in_specs=[SMEM] * 3
        + pair_specs(pairs, state_shapes + [goal.shape[1:]], pl.Buffered(1))
        + whole_specs(pairs, [vector.shape for vector in vectors])
        + [VMEM_BLOCK] * 5,
        out_specs=pair_specs(pairs, [(AREA, WIDE)] + BACK) + whole_specs(pairs, out_shapes),
        out_shape=pair_arrays(pairs, [(AREA, WIDE)] + BACK, [f32] * 4)
        + [make(shape, kind) for shape, kind in zip(out_shapes, (bf16, bf16, f32))],
        scratch_shapes=scratch,
        compiler_params=pltpu.CompilerParams(
            vmem_limit_bytes=(40 if pairs == 1 else 56) * 1024 * 1024,
            fuse_transposed_lhs_in_matmul=True,
        ),
        name="blocks",
    )(*places, sizes, inv, mix, stat, goal, *vectors, *weights)


def exit_kernel(
    pairs,
    strip_count,
    size_ref,
    x_in,
    inv_in,
    pool_in,
    mix_in,
    stat_in,
    zed_in,
    dx_in,
    mean_in,
    flat_ref,
    vec_two_ref,
    payload_hbm,
    vector_ref,
    payload_ref,
    image_ref,
    col_ref,
    dx_ref,
    back_ref,
    acc_ref,
    sem,
):
    pair = pl.program_id(0) if pairs > 1 else 0
    x_ref, inv_ref, pool_ref, mix_ref, stat_ref, zed_ref, low_ref, mean_ref = (
        ref.at[0] for ref in (x_in, inv_in, pool_in, mix_in, stat_in, zed_in, dx_in, mean_in)
    )
    shape = Geometry(size_ref, pair)
    count_two = shape.count_two
    gain1, bias1, scale1, gain2 = (vec_two_ref[n : n + 1] for n in range(4))
    mean1, scaling1, mean2, scaling2 = (stat_ref[n] for n in range(4))
    normal2 = (scaling2, -mean2 * scaling2)
    clear_edges(col_ref)
    nothing = jnp.zeros((8, C2), f32)
    back_gain2 = scaling2 * gain2
    back_mean2 = -scaling2 * mean_ref[0]
    back_normal2 = scaling2 * mean_ref[1]

    if pairs > 1:

        @pl.when(pair == 0)
        def _():
            acc_ref[...] = jnp.zeros(acc_ref.shape, f32)

    def add_up(n, total):
        acc_ref[n] = total if pairs == 1 else acc_ref[n] + total

    def unmix(k, d_scale):
        rows = step_rows(k)
        for pr in range(2):
            weighted = []
            for pc in range(2):
                plane = pr * 2 + pc
                share = inv_ref[plane, rows]
                normal = affine(mix_ref[plane, rows], *normal2)
                back = affine(low_ref[plane, rows], back_gain2, back_mean2)
                back = back - scaled(normal, back_normal2)
                d_mixed = jnp.where(share > 0.0, zed_ref[plane, rows] + back, 0.0)
                dx_ref[plane, rows] = d_mixed
                d_scale = d_scale + fold(pool_ref[plane, rows] * d_mixed)
                weighted.append(scale1 * d_mixed * share)
            put_col_windows(col_ref, pr, k, *weighted)
        return d_scale

    add_up(2, sweep(unmix, nothing))
    normal1 = (spread(scaling1, C2), spread(-mean1 * scaling1, C2))

    def unpool(k, carry):
        d_shift, d_gain = carry
        rows = step_rows(k)
        for pc in range(2):
            windows = row_windows(col_ref, pc, k)
            for pr in range(2):
                plane = pr * 2 + pc
                valid = inv_ref[plane, rows] > 0.0
                d_normal = windows[pr] - scale1 * dx_ref[plane, rows]
                d_normal = jnp.where(valid, d_normal, 0.0)
                back_ref[plane, rows] = d_normal
                normal = affine(x_ref[plane, rows], *normal1)
                d_shift = d_shift + fold(d_normal)
                d_gain = d_gain + fold(d_normal * normal)
        return (d_shift, d_gain)

    d_shift, d_gain = sweep(unpool, (nothing, nothing))
    add_up(1, d_shift)
    add_up(0, d_gain)
    mean_shift = by_image(d_shift * gain1) / count_two
    mean_gain = by_image(d_gain * gain1) / count_two
    back_gain1 = scaling1 * gain1
    back_mean1 = spread(-scaling1 * mean_shift, C2)
    back_normal1 = spread(scaling1 * mean_gain, C2)

    def unnorm(k, carry):
        rows = step_rows(k)
        for plane in range(4):
            normal = affine(x_ref[plane, rows], *normal1)
            back = affine(back_ref[plane, rows], back_gain1, back_mean1)
            back = back - scaled(normal, back_normal1)
            valid = inv_ref[plane, rows] > 0.0
            dx_ref[plane, rows] = jnp.where(valid, dx_ref[plane, rows] + back, 0.0)
        return carry

    sweep(unnorm, 0)

    def give_back(image, plane, line_place, there):
        image_ref[image, there] = dx_ref[plane, line_place]

    image_ref[...] = jnp.zeros(image_ref.shape, f32)
    each_image(size_ref, pair, give_back)

    def from_rows(within, carry):
        for spot in range(2 * STRIPS):
            image, strip = spot // STRIPS, spot % STRIPS
            start = pl.multiple_of((strip * SR + within) * LINE, LINE)
            target = strip_place(pair, spot, strip_count)
            payload_ref[target, within] = image_ref[image, pl.ds(start, CW)].astype(bf16)
        return carry

    lax.fori_loop(0, SR, from_rows, 0)

    def finish():
        copy = pltpu.make_async_copy(payload_ref, payload_hbm, sem)
        copy.start()
        vector_ref[...] = flat_ref[...]
        for n in range(3):
            vector_ref[n : n + 1] = jnp.sum(acc_ref[n], axis=0, keepdims=True)
        copy.wait()

    if pairs == 1:
        finish()
    else:
        pl.when(pair == pairs - 1)(finish)


def run_exit(sizes, state, back, flat, vec_two, strip_count):
    pairs = strip_count // 8
    payload = (strip_count, SR, CW, C2)
    make = pltpu.VMEM if pairs == 1 else jax.ShapeDtypeStruct
    plane_f32 = pltpu.VMEM((4, AREA, C2), f32)
    arrays = [*state, *back]
    if pairs == 1:
        arrays = held_in(pltpu.VMEM, *arrays)
    return pl.pallas_call(
        functools.partial(exit_kernel, pairs, strip_count),
        grid=() if pairs == 1 else (pairs,),
        in_specs=[SMEM]
        + pair_specs(pairs, STATE + BACK, pl.Buffered(1))
        + whole_specs(pairs, [flat.shape, vec_two.shape]),
        out_specs=[HBM] + whole_specs(pairs, [flat.shape]),
        out_shape=[pltpu.HBM(payload, bf16), make(flat.shape, f32)],
        scratch_shapes=[
            pltpu.VMEM(payload, bf16),
            pltpu.VMEM((2, CH * LINE, C2), f32),
            pltpu.VMEM((4, AREA + 2 * LINE, C2), f32),
            plane_f32,
            plane_f32,
            pltpu.VMEM((3, 8, C2), f32),
            pltpu.SemaphoreType.DMA,
        ],
        compiler_params=roomy(8 if pairs == 1 else 40),
        name="exit",
    )(sizes, *arrays, flat, vec_two)


def pack_kernel(master_ref, dense_ref):
    values = master_ref[...]
    dense_ref[...] = jnp.concatenate([values[:, :HALF], values[:, HALF:]], axis=2).astype(bf16)


def pack(master):
    owned = master.shape[0]
    return pl.pallas_call(
        pack_kernel,
        out_shape=jax.ShapeDtypeStruct((owned, HALF, 2 * BS), bf16),
        name="pack",
    )(master)


def fold_pair_kernel(near_ref, got_ref, own_ref, *part_refs):
    share = own_ref.shape[0]

    def one(n, carry):
        for k in range(len(part_refs) + 1):
            total = near_ref[k * share + n].astype(f32) + got_ref[k * share + n].astype(f32)
            if k == 0:
                own_ref[n] = total
            else:
                part_refs[k - 1][n] = total.astype(bf16)
        return carry

    lax.fori_loop(0, share, one, 0, unroll=4)


def fold_pair(near, got, groups):
    shape = ((near.shape[0] - 1) // groups,) + near.shape[1:]
    return pl.pallas_call(
        fold_pair_kernel,
        in_specs=[VMEM_BLOCK] * 2,
        out_specs=[VMEM_BLOCK] * groups,
        out_shape=[pltpu.VMEM(shape, f32)] + [pltpu.VMEM(shape, bf16)] * (groups - 1),
        compiler_params=roomy(4),
        name="fold_pair",
    )(*held_in(pltpu.VMEM, near, got))


def fold_tile_kernel(pieces, spot_ref, *refs):
    piece_refs, refs = refs[:pieces], refs[pieces:]
    vector_refs, refs = refs[:pieces], refs[pieces:]
    out_refs, sum_ref = refs[:-1], refs[-1]
    groups = len(out_refs)
    share = out_refs[0].shape[0]
    owned = piece_refs[0].shape[0]
    total = vector_refs[0][...]
    for ref in vector_refs[1:]:
        total = total + ref[...]
    for n in range(sum_ref.shape[0]):
        sum_ref[n] = jnp.zeros((HALF, 128), f32)
    for n in range(VEC_BLOCKS):
        sum_ref[n] = total[n * HALF : (n + 1) * HALF]

    def one(n, carry):
        for k, out_ref in enumerate(out_refs):
            number = lax.rem(spot_ref[0] + k, groups) * share + n
            block = jnp.minimum(number, owned - 1)
            total = piece_refs[0][block].astype(f32)
            for ref in piece_refs[1:]:
                total = total + ref[block].astype(f32)
            rest = sum_ref[jnp.maximum(number - owned, 0)]
            out_ref[n] = jnp.where(number < owned, total, rest).astype(out_ref.dtype)
        return carry

    lax.fori_loop(0, share, one, 0, unroll=share <= 16)


def fold_tile(spot, pieces, vectors, extra, groups):
    shape = ((pieces[0].shape[0] + extra) // groups,) + pieces[0].shape[1:]
    return pl.pallas_call(
        functools.partial(fold_tile_kernel, len(pieces)),
        in_specs=[SMEM] + [VMEM_BLOCK] * (len(pieces) + len(vectors)),
        out_specs=[VMEM_BLOCK] * groups,
        out_shape=[pltpu.VMEM(shape, f32)] + [pltpu.VMEM(shape, bf16)] * (groups - 1),
        scratch_shapes=[pltpu.VMEM((extra, HALF, 128), f32)],
        compiler_params=roomy(8),
        name="fold_tile",
    )(spot, *held_in(pltpu.VMEM, *pieces, *vectors))


def fold_batch_kernel(owned, vector_weight, spot_ref, *refs):
    part_refs, (total_ref, norm_ref) = refs[:-2], refs[-2:]
    share = total_ref.shape[0]
    square = jnp.zeros((8, 128), f32)
    for n in range(share):
        total = part_refs[0][n].astype(f32)
        for ref in part_refs[1:]:
            total = total + ref[n].astype(f32)
        total_ref[n] = total.astype(bf16)
        weight = jnp.where(spot_ref[0] * share + n < owned, 1.0, vector_weight)
        square = square + weight * fold(total * total)
    square = jnp.sum(jnp.sum(square, axis=1, keepdims=True), axis=0, keepdims=True)
    norm_ref[...] = jnp.broadcast_to(square[None], norm_ref.shape)


def fold_batch(spot, parts, owned, tile_count):
    count = tile_count * len(parts)
    return pl.pallas_call(
        functools.partial(fold_batch_kernel, owned, 1.0 / tile_count),
        in_specs=[SMEM] + [VMEM_BLOCK] * len(parts),
        out_specs=[VMEM_BLOCK] * 2,
        out_shape=[pltpu.VMEM(parts[0].shape, bf16), pltpu.VMEM((count, 1, 128), f32)],
        name="fold_batch",
    )(spot, *held_in(pltpu.VMEM, *parts))


def copies_between(sources, targets, sems, owned):
    return [
        [
            pltpu.make_async_copy(
                source.at[pl.ds(first, min(8, owned - first))],
                target.at[pl.ds(first, min(8, owned - first))],
                sems.at[len(sources) * n + k],
            )
            for k, (source, target) in enumerate(zip(sources, targets))
        ]
        for n, first in enumerate(range(0, owned, 8))
    ]


def groups_of(owned):
    return [(first, min(4, owned - first)) for first in range(0, owned, 4)]


def diagonal_of(count):
    order = (count * BS, count * BS)
    return lax.broadcasted_iota(jnp.int32, order, 0) // BS == (
        lax.broadcasted_iota(jnp.int32, order, 1) // BS
    )


def gather_kernel(owned, groups, spot_ref, *refs):
    quarters, refs = refs[:groups], refs[groups:]
    stat_hbm, stat_refs, refs = refs[:5], refs[5:10], refs[10:]
    grad_ref, left_ref, right_ref, vector_ref, in_sem = refs
    share = quarters[0].shape[0]
    copies = copies_between(stat_hbm, stat_refs, in_sem, owned)
    for arriving in copies:
        for copy in arriving:
            copy.start()
    left_half = lax.broadcasted_iota(jnp.int32, (HALF, 128), 1) < BS

    def summed(number):
        source = number // share
        local = number - source * share
        turn = lax.rem(spot_ref[0] - source + groups, groups)
        value = quarters[0][local].astype(f32)
        for k in range(1, groups):
            value = jnp.where(turn == k, quarters[k][local].astype(f32), value)
        return value

    for n in range(vector_ref.shape[0]):
        vector_ref[n] = summed(owned + n)
    for first, count in groups_of(owned):
        sides = []
        for n in range(first, first + count, 2):
            dense = summed(n)
            turned = pltpu.roll(dense, BS, 1)
            if n + 1 < first + count:
                second = summed(n + 1)
                top = jnp.where(left_half, dense, pltpu.roll(second, BS, 1))
                low = jnp.where(left_half, turned, second)
                side = jnp.concatenate([top, low], axis=0)
                grad_ref[n + 1] = pltpu.roll(side, BS, 1)[:, :BS]
            else:
                side = jnp.concatenate([dense, turned], axis=0)[:, :BS]
            grad_ref[n] = side[:, :BS]
            sides.append(side.astype(bf16))
        wide = jnp.concatenate(sides, axis=1)
        here = pl.ds(first, count)
        tall = jnp.where(diagonal_of(count), jnp.concatenate([wide] * count, axis=0), 0.0)
        left_ref[here] = product_nt(tall, wide).reshape(count, BS, BS)
        right = product_tn(wide, wide)
        for n in range(count):
            at = n // 2 * 128
            block = right[n * BS : n * BS + BS, at : min(at + 128, count * BS)]
            if n % 2:
                block = pltpu.roll(block, BS, 1)
            right_ref[first + n] = block[:, :BS]
    for arriving in copies:
        for copy in arriving:
            copy.wait()


def gather(spot, quarters, extra, *stats):
    shape = stats[0].shape
    groups = len(quarters)
    square = pltpu.VMEM(shape, f32)
    return pl.pallas_call(
        functools.partial(gather_kernel, shape[0], groups),
        in_specs=[SMEM] + [VMEM_BLOCK] * groups + [HBM] * 5,
        out_specs=[VMEM_BLOCK] * 9,
        out_shape=[square] * 8 + [pltpu.VMEM((extra, HALF, 128), f32)],
        scratch_shapes=[pltpu.SemaphoreType.DMA((5 * -(-shape[0] // 8),))],
        compiler_params=roomy(8),
        name="gather",
    )(spot, *held_in(pltpu.VMEM, *quarters), *held_in(pltpu.HBM, *stats))


def update_kernel(owned, *refs):
    norm_ref, stat_refs, (sum_ref, left_sum, right_sum, vector_sum) = refs[0], refs[1:6], refs[6:10]
    out_hbm, vector_ref, clip_ref, out_refs, out_sem = (
        refs[10:15],
        refs[15],
        refs[16],
        refs[17:22],
        refs[22],
    )
    master_ref, left_stat_ref, right_stat_ref, left_root_ref, right_root_ref = stat_refs
    grad_ref, left_ref, right_ref, new_ref, copy_ref = out_refs
    norm = jnp.sqrt(jnp.sum(norm_ref[...], axis=0))
    factor = jnp.minimum(1.0, clip_limit / norm)
    clip_ref[...] = norm
    vector_ref[...] = vector_sum[...] * factor
    factor = factor[:, :BS]
    copies = copies_between(out_refs, out_hbm, out_sem, owned)
    for first, count in groups_of(owned):
        here = pl.ds(first, count)
        grad = sum_ref[here] * factor
        grad_ref[here] = grad
        left_ref[here] = 0.5 * left_stat_ref[here] + left_sum[here] * factor * (0.5 * factor)
        right_ref[here] = 0.5 * right_stat_ref[here] + right_sum[here] * factor * (0.5 * factor)
        order = count * BS
        roots = left_root_ref[here].reshape(order, BS).astype(bf16)
        low = [grad[n].astype(bf16) for n in range(count)]
        wide = jnp.concatenate(low, axis=1)
        stepped = jnp.where(diagonal_of(count), product(roots, wide), 0.0).astype(bf16)
        roots = right_root_ref[here].reshape(order, BS).astype(bf16)
        stepped = product(stepped, roots).reshape(count, BS, BS)
        new = master_ref[here] - rate_matrix * stepped
        new_ref[here] = new
        copy_ref[here] = new.astype(bf16)
        if (first + count) % 8 == 0 or first + count == owned:
            for copy in copies[first // 8]:
                copy.start()
    for leaving in copies:
        for copy in leaving:
            copy.wait()


def update(norm, *arrays):
    shape = arrays[0].shape
    types = [f32] * 4 + [bf16]
    return pl.pallas_call(
        functools.partial(update_kernel, shape[0]),
        in_specs=[VMEM_BLOCK] * 10,
        out_specs=[HBM] * 5 + [VMEM_BLOCK] * 2,
        out_shape=[pltpu.HBM(shape, kind) for kind in types]
        + [
            jax.ShapeDtypeStruct(arrays[-1].shape, f32),
            jax.ShapeDtypeStruct((1, 128), f32),
        ],
        scratch_shapes=[pltpu.VMEM(shape, kind) for kind in types]
        + [pltpu.SemaphoreType.DMA((5 * -(-shape[0] // 8),))],
        compiler_params=roomy(12),
        name="update",
    )(*held_in(pltpu.VMEM, norm, *arrays))


def share_out(pieces, axis):
    return lax.all_to_all(pieces, axis, split_axis=0, concat_axis=0, tiled=True)


def swap(piece, distance):
    count = lax.axis_size("tile")
    return lax.ppermute(piece, "tile", [(i, i ^ distance) for i in range(count)])


def on_device(
    pixels,
    buckets,
    slot_owner_table,
    out_grad,
    master,
    left_stat,
    right_stat,
    left_root,
    right_root,
    vectors,
    moment,
):
    tile_count = lax.axis_size("tile")
    tile_place = lax.axis_index("tile")
    slot_count = pixels.shape[2]
    group_count = tile_count // STRIPS
    pairs = group_count // 2
    owned = master.shape[0]
    slots = owned * tile_count
    batch_count = lax.axis_size("batch")
    spot = lax.axis_index("batch").astype(jnp.int32).reshape(1)
    extra = extra_of(owned, batch_count)
    strips = share_out(pixels.reshape((tile_count,) + pixels.shape[3:]), "tile")
    dense = pack(master)
    paired = tile_count <= 8
    if paired:
        mine = [dense] + [swap(dense, 2 * k) for k in range(1, tile_count // 2)]
        pieces = mine + [swap(piece, 1) for piece in mine]
    else:
        pieces = [lax.all_gather(dense, "tile", axis=0, tiled=True)]

    numbers = jnp.arange(slots, dtype=jnp.int32)
    slot_of = jnp.sum(
        jnp.where(slot_owner_table[None, :] == numbers[:, None], numbers[None, :], 0), axis=1
    )
    owner = slot_of // owned
    within = slot_of - owner * owned
    place_of = slot_of
    if paired:
        apart = owner ^ tile_place
        apart = (apart & 1) * (tile_count // 2) + (apart >> 1)
        slot_of = place_of = within + owned * apart
    half = slots // 2
    near_place = jnp.where(place_of < half, place_of, half)
    far_place = jnp.where(place_of < half, half, place_of - half)
    image_ids = lax.dynamic_index_in_dim(
        buckets.reshape(group_count, slot_count), tile_place, 1, keepdims=False
    )
    turned = image_ids >= 2
    heights = jnp.where(image_ids == 0, 5 * CH // 9, jnp.where(image_ids == 1, 7 * CH // 9, CH))
    breadths = jnp.where(image_ids == 0, CW, jnp.where(image_ids == 1, 7 * CW // 9, 5 * CW // 9))
    sizes = jnp.stack(
        [
            jnp.where(turned, breadths, heights),
            jnp.where(turned, heights, breadths),
            turned,
        ],
        axis=1,
    )
    sizes = sizes.reshape(-1).astype(jnp.int32)

    two = 6 * C2 + HID2 + C2
    vec_two = jnp.concatenate([vectors[: 6 * C2], vectors[6 * C2 + HID2 : two]]).reshape(7, C2)
    vec_hid_two = vectors[6 * C2 : 6 * C2 + HID2].reshape(1, HID2)
    wide_end = two + 7 * C3
    vec_three = jnp.concatenate([vectors[two:wide_end], vectors[wide_end + HID3 :]])
    vec_three = jnp.pad(vec_three.reshape(8, C3), ((0, 0), (0, WIDE - C3)))
    vec_hid_three = vectors[wide_end : wide_end + HID3].reshape(1, HID3)

    flips = turned.reshape(-1, 1, 1, 1)
    goal = out_grad.reshape(2 * pairs, H3, W3, C3)
    goal = jnp.where(flips, goal.transpose(0, 2, 1, 3), goal)[:, :LINES]
    goal = goal.reshape(pairs, 2, LINES, W3, C3).transpose(0, 2, 3, 1, 4)
    goal = goal.reshape(pairs, LINES, 2 * W3, C3)
    goal = jnp.pad(goal, ((0, 0), (0, 0), (0, LINE - 2 * W3), (0, WIDE - C3)))
    goal = goal.reshape(pairs, AREA, WIDE)

    weights = run_unpack(slot_of, pieces)
    state = run_entry(sizes, strips, vec_two)
    result, *back, near, far, flat = run_main(
        (near_place, far_place),
        sizes,
        state,
        goal,
        (vec_two, vec_hid_two, vec_three, vec_hid_three),
        weights,
        tile_count,
    )
    pixel_back, vector = run_exit(sizes, state, back, flat, vec_two, tile_count)
    if paired:
        own, *parts = fold_pair(near, swap(far, 1), tile_count // 2)
        pieces = [own] + [swap(part, 2 * k + 2) for k, part in enumerate(parts)]
        vector, _ = lax.optimization_barrier((vector, parts[0]))
        vector = vector + swap(vector, 1)
        vectors_in = [vector] + [swap(vector, 2 * k) for k in range(1, tile_count // 2)]
    else:
        outgoing = jnp.concatenate([near[:half], far[:half]], axis=0)
        pieces = list(share_out(outgoing.reshape(tile_count, owned, HALF, 128), "tile"))
        vectors_in = list(lax.all_gather(vector, "tile"))
    result, pieces[1] = lax.optimization_barrier((result, pieces[1]))
    result = result.reshape(pairs, LINES, LINE, WIDE)[:, :, : 2 * W3, :C3]
    result = result.reshape(pairs, LINES, W3, 2, C3).transpose(0, 3, 1, 2, 4)
    result = result.reshape(2 * pairs, LINES, W3, C3)
    result = jnp.pad(result, ((0, 0), (0, H3 - LINES), (0, 0), (0, 0)))
    result = jnp.where(flips, result.transpose(0, 2, 1, 3), result)
    result = result.reshape(out_grad.shape)
    result, vectors_in[0] = lax.optimization_barrier((result, vectors_in[0]))
    own, *parts = fold_tile(spot, pieces, vectors_in, extra, batch_count)
    pixel_back, parts[0] = lax.optimization_barrier((pixel_back, parts[0]))
    returned = share_out(pixel_back, "tile")
    parts = [
        lax.ppermute(part, "batch", [(i, (i + k + 1) % batch_count) for i in range(batch_count)])
        for k, part in enumerate(parts)
    ]
    quarter, norm = fold_batch(spot, [own] + parts, owned, tile_count)
    quarters = [quarter] + [
        lax.ppermute(quarter, "batch", [(i, (i + k) % batch_count) for i in range(batch_count)])
        for k in range(1, batch_count)
    ]
    returned, norm = lax.optimization_barrier((returned, norm))
    norm = share_out(norm, ("batch", "tile"))
    returned = returned.astype(f32).reshape(pixels.shape)
    gathered = gather(
        spot, quarters, extra, master, left_stat, right_stat, left_root, right_root
    )
    block_grad, left_new, right_new, master_new, weight_copy, whole_vector, clip = update(
        norm, *gathered
    )
    clip_norm = clip[0, 0]
    share = vectors.shape[0] // tile_count
    whole_vector = whole_vector.reshape(-1)
    vec_grad = lax.dynamic_slice_in_dim(whole_vector, tile_place * share, share, 0)
    vec_moment = moment + vec_grad * vec_grad
    own_vectors = lax.dynamic_slice_in_dim(vectors, tile_place * share, share, 0)
    vec_new = own_vectors - rate_vector * vec_grad / (jnp.sqrt(vec_moment) + eps_adagrad)
    return (
        result,
        returned,
        clip_norm,
        block_grad,
        left_new,
        right_new,
        master_new,
        weight_copy,
        vec_grad,
        vec_moment,
        vec_new,
    )


def solution(mesh):
    placed = (
        P("batch", "tile", None, None, None, None),
        P("batch"),
        P(),
        P("batch", "tile", None, None, None, None, None),
        P("tile", None, None),
        P("tile", None, None),
        P("tile", None, None),
        P("tile", None, None),
        P("tile", None, None),
        P(),
        P("tile"),
    )
    return jax.shard_map(
        on_device,
        mesh=mesh,
        in_specs=placed,
        out_specs=(
            P("batch", "tile", None, None, None, None, None),
            P("batch", "tile", None, None, None, None),
            P(),
            P("tile", None, None),
            P("tile", None, None),
            P("tile", None, None),
            P("tile", None, None),
            P("tile", None, None),
            P("tile"),
            P("tile"),
            P("tile"),
        ),
        check_vma=False,
    )
```

```python
import functools

import jax
import jax.numpy as jnp
from jax import lax
from jax.experimental import pallas as pl
from jax.experimental.pallas import tpu as pltpu
from jax.sharding import PartitionSpec as P

C2 = 128
HID2 = 512
C3 = 320
HID3 = 1280
CH = 36
CW = 36
STRIPS = 4
BS = 64
SR = CH // STRIPS
H3 = CH // 2
W3 = CW // 2
LONG = 7 * CH // 9
LINES = LONG // 2
WIDE = 384
LINE = 40
AREA = LINES * LINE
STEP = 2 * LINE
STEPS = AREA // STEP
HALF = BS // 2

eps_norm = 1e-05
clip_limit = 1.0
rate_matrix = 0.3
rate_vector = 0.3
eps_adagrad = 1e-08
f32 = jnp.float32
bf16 = jnp.bfloat16

SHAPES = [(C2, HID2), (HID2, C2), (9 * C2, C3), (C3, HID3), (HID3, C3)]
USED = sum(rows // BS * (cols // BS) for rows, cols in SHAPES)
VEC_ROWS = (6 * C2 + HID2 + C2 + C3 + 6 * C3 + HID3 + C3) // 128


VEC_BLOCKS = -(-VEC_ROWS // HALF)


def extra_of(owned, groups):
    return VEC_BLOCKS + -(owned + VEC_BLOCKS) % groups


def product(left, right):
    return jnp.dot(left, right, preferred_element_type=f32)


def product_nt(left, right):
    return lax.dot_general(left, right, (((1,), (1,)), ((), ())), preferred_element_type=f32)


def product_tn(left, right):
    return lax.dot_general(left, right, (((0,), (0,)), ((), ())), preferred_element_type=f32)


def gelu_pair(values):
    bell = jnp.exp2(values * values * (-0.5 * 1.4426950408889634))
    step = pl.reciprocal(1.0 + (0.3275911 * 0.7071067811865476) * jnp.abs(values), approx=True)
    tail = step * (
        0.5 * 0.254829592
        + step
        * (
            0.5 * -0.284496736
            + step
            * (0.5 * 1.421413741 + step * (0.5 * -1.453152027 + step * (0.5 * 1.061405429)))
        )
    )
    tail = tail * bell
    share = jnp.where(values >= 0.0, 1.0 - tail, tail)
    return (values * share, share + values * (bell * 0.3989422804014327))


def fold(values):
    chans = values.shape[-1]
    return jnp.sum(values.reshape(-1, 8, chans), axis=0)


def by_image(total):
    total = total + pltpu.roll(total, 4, 0)
    total = total + pltpu.roll(total, 2, 0)
    return jnp.sum(total, axis=1, keepdims=True)


def line(pattern):
    return jnp.concatenate([pattern] * (LINE // 8), axis=0)


def spread(pattern, chans):
    return jnp.broadcast_to(pattern, (8, chans))


def affine(values, factor, shift):
    tiles = values.reshape(-1, 8, values.shape[-1])
    return (tiles * factor + shift).reshape(values.shape)


def scaled(values, factor):
    tiles = values.reshape(-1, 8, values.shape[-1])
    return (tiles * factor).reshape(values.shape)


def from_left(values):
    return pltpu.roll(values, 2, 0)


def from_right(values):
    return pltpu.roll(values, values.shape[0] - 2, 0)


def rounded(values):
    return values.astype(bf16).astype(f32)


def widen(values):
    return jnp.concatenate([values] * (WIDE // 128), axis=-1)


def norm_terms(total, square, count):
    mean = by_image(total) / count
    scaling = lax.rsqrt(by_image(square) / count - mean * mean + eps_norm)
    return (mean, scaling)


def sweep(visit, start):
    return lax.fori_loop(0, STEPS, visit, start, unroll=True)


def step_rows(k, lines=0):
    start = k * STEP + lines * LINE
    return pl.ds(start if isinstance(k, int) else pl.multiple_of(start, LINE), STEP)


def held_in(space, *arrays):
    return [pltpu.with_memory_space_constraint(array, space) for array in arrays]


VMEM_BLOCK = pl.BlockSpec(memory_space=pltpu.VMEM)
HBM = pl.BlockSpec(memory_space=pltpu.HBM)
SMEM = pl.BlockSpec(memory_space=pltpu.SMEM)


def roomy(mebibytes):
    return pltpu.CompilerParams(vmem_limit_bytes=mebibytes * 1024 * 1024)


class Geometry:
    def __init__(self, size_ref, pair):
        parity = lax.broadcasted_iota(jnp.int32, (8, 128), 0) % 2
        high, broad, turned = (
            jnp.where(parity == 0, size_ref[pair * 6 + n], size_ref[pair * 6 + 3 + n])
            for n in range(3)
        )
        self.high = high
        self.count_two = (high * broad * C2).astype(f32)[:, :1]
        self.high3 = (high + 1) // 2
        broad3 = (broad + 1) // 2
        self.count_three = (self.high3 * broad3 * C3).astype(f32)[:, :1]
        place = lax.broadcasted_iota(jnp.int32, (LINE, 128), 0) // 2
        inside = lax.broadcasted_iota(jnp.int32, (LINE, 128), 0) < 2 * W3
        self.reach = []
        self.col_share = []
        for pc in range(2):
            column = 2 * place + pc
            self.reach.append(jnp.where(inside & (column < line(broad)), line(high), 0))
            edge = (column == 0) | (column == line(broad) - 1)
            self.col_share.append(jnp.where(edge, 0.5, 1.0 / 3.0))
        self.reach3 = jnp.where(inside & (place < line(broad3)), line(self.high3), 0)
        edge3 = (place == 0) | (place == line(broad3) - 1)
        self.col_share3 = jnp.where(edge3, 0.5, 1.0 / 3.0)
        self.flipped = jnp.concatenate([turned] * (STEP // 8), axis=0) > 0

    def share(self, plane, k):
        pr, pc = plane // 2, plane % 2
        return self.lines(4 * k + pr, 2, self.reach[pc], self.col_share[pc], self.high)

    def share3(self, k):
        return self.lines(2 * k, 1, self.reach3, self.col_share3, self.high3)

    def lines(self, row, stride, reach, col_share, height):
        parts = []
        for n in range(2):
            here = row + stride * n
            row_share = jnp.where((here == 0) | (here == height - 1), 0.5, 1.0 / 3.0)
            parts.append(jnp.where(here < reach, line(row_share) * col_share, 0.0))
        return jnp.concatenate(parts, axis=0)


def strip_place(pair, spot, strip_count):
    return lax.rem(pair * 8 + strip_count - 2 + spot, strip_count)


def each_image(size_ref, pair, visit):
    for image in range(2):
        way = size_ref[pair * 6 + 3 * image + 2]
        for flat in (True, False):

            @pl.when(way == (0 if flat else 1))
            def _():
                def one(r, carry):
                    for pr in range(2):
                        for pc in range(2):
                            line_place = pl.ds(r * LINE + image, W3, stride=2)
                            if flat:
                                there = pl.ds((2 * r + pr) * LINE + pc, W3, stride=2)
                            else:
                                there = pl.ds(pc * LINE + 2 * r + pr, W3, stride=2 * LINE)
                            visit(image, pr * 2 + pc, line_place, there)
                    return carry

                lax.fori_loop(0, LINES, one, 0)


def row_windows(col_ref, pc, k):
    both = col_ref[pc, step_rows(k, 1)] + col_ref[2 + pc, step_rows(k, 1)]
    return (both + col_ref[2 + pc, step_rows(k)], both + col_ref[pc, step_rows(k, 2)])


def put_col_windows(col_ref, pr, k, even, odd):
    both = even + odd
    col_ref[pr * 2, step_rows(k, 1)] = both + from_left(odd)
    col_ref[pr * 2 + 1, step_rows(k, 1)] = both + from_right(even)


def clear_edges(col_ref):
    zero_line = jnp.zeros((LINE, C2), f32)
    for plane in range(4):
        col_ref[plane, 0:LINE] = zero_line
        col_ref[plane, AREA + LINE : AREA + 2 * LINE] = zero_line


def entry_kernel(
    pairs,
    strip_count,
    size_ref,
    strips_ref,
    vec_two_ref,
    x_out,
    inv_out,
    pool_out,
    mix_out,
    stat_out,
    image_ref,
    col_ref,
):
    pair = pl.program_id(0) if pairs > 1 else 0
    x_ref, inv_ref, pool_ref, mix_ref = (ref.at[0] for ref in (x_out, inv_out, pool_out, mix_out))
    shape = Geometry(size_ref, pair)
    gain1, bias1, scale1 = (vec_two_ref[n : n + 1] for n in range(3))
    clear_edges(col_ref)

    def to_rows(within, carry):
        for spot in range(2 * STRIPS):
            image, strip = spot // STRIPS, spot % STRIPS
            start = pl.multiple_of((strip * SR + within) * LINE, LINE)
            source = strip_place(pair, spot, strip_count)
            image_ref[image, pl.ds(start, CW)] = strips_ref[source, within].astype(f32)
        return carry

    lax.fori_loop(0, SR, to_rows, 0)

    def take_in(image, plane, line_place, there):
        x_ref[plane, line_place] = image_ref[image, there]

    each_image(size_ref, pair, take_in)

    def arrange(k, carry):
        total, square = carry
        rows = step_rows(k)
        for plane in range(4):
            share = shape.share(plane, k)
            inv_ref[plane, rows] = share
            values = jnp.where(share > 0.0, x_ref[plane, rows], 0.0)
            x_ref[plane, rows] = values
            total = total + fold(values)
            square = square + fold(values * values)
        return (total, square)

    nothing = jnp.zeros((8, C2), f32)
    total, square = sweep(arrange, (nothing, nothing))
    mean1, scaling1 = norm_terms(total, square, shape.count_two)
    factor1 = scaling1 * gain1
    shift1 = bias1 - mean1 * scaling1 * gain1

    def window_cols(k, carry):
        rows = step_rows(k)
        for pr in range(2):
            masked = []
            for pc in range(2):
                plane = pr * 2 + pc
                normal = rounded(affine(x_ref[plane, rows], factor1, shift1))
                masked.append(jnp.where(inv_ref[plane, rows] > 0.0, normal, 0.0))
            put_col_windows(col_ref, pr, k, *masked)
        return carry

    sweep(window_cols, 0)

    def mix(k, carry):
        total, square = carry
        rows = step_rows(k)
        for pc in range(2):
            windows = row_windows(col_ref, pc, k)
            for pr in range(2):
                plane = pr * 2 + pc
                values = x_ref[plane, rows]
                share = inv_ref[plane, rows]
                pooled = windows[pr] * share - rounded(affine(values, factor1, shift1))
                pooled = jnp.where(share > 0.0, pooled, 0.0)
                mixed = values + scale1 * pooled
                pool_ref[plane, rows] = pooled
                mix_ref[plane, rows] = mixed
                total = total + fold(mixed)
                square = square + fold(mixed * mixed)
        return (total, square)

    total, square = sweep(mix, (nothing, nothing))
    mean2, scaling2 = norm_terms(total, square, shape.count_two)
    for n, value in enumerate((mean1, scaling1, mean2, scaling2)):
        stat_out[0, n] = spread(value, 128)


def pair_specs(pairs, shapes, mode=None):
    if pairs == 1:
        return [VMEM_BLOCK] * len(shapes)
    return [
        pl.BlockSpec(
            (1,) + shape, lambda t, rank=len(shape): (t,) + (0,) * rank, pipeline_mode=mode
        )
        for shape in shapes
    ]


def whole_specs(pairs, shapes):
    if pairs == 1:
        return [VMEM_BLOCK] * len(shapes)
    return [
        pl.BlockSpec(
            shape,
            lambda t, rank=len(shape): (0,) * rank,
            pipeline_mode=pl.Buffered(1),
        )
        for shape in shapes
    ]


def pair_arrays(pairs, shapes, kinds):
    make = pltpu.VMEM if pairs == 1 else jax.ShapeDtypeStruct
    return [make((pairs,) + shape, kind) for shape, kind in zip(shapes, kinds)]


STATE = [(4, AREA, C2)] * 4 + [(4, 8, 128)]
BACK = [(4, AREA, C2)] * 2 + [(2, 8, 128)]


def run_entry(sizes, strips, vec_two):
    strip_count = strips.shape[0]
    pairs = strip_count // 8
    return pl.pallas_call(
        functools.partial(entry_kernel, pairs, strip_count),
        grid=() if pairs == 1 else (pairs,),
        in_specs=[SMEM] + whole_specs(pairs, [strips.shape, vec_two.shape]),
        out_specs=pair_specs(pairs, STATE),
        out_shape=pair_arrays(pairs, STATE, [f32] * 5),
        scratch_shapes=[
            pltpu.VMEM((2, CH * LINE, C2), f32),
            pltpu.VMEM((4, AREA + 2 * LINE, C2), f32),
        ],
        compiler_params=roomy(6 if pairs == 1 else 40),
        name="entry",
    )(sizes, strips, vec_two)


WEIGHTS = [(C2, HID2), (HID2, C2), (9 * C2, WIDE), (WIDE, HID3), (HID3, WIDE)]


def unpack_kernel(piece_count, slot_ref, *refs):
    piece_refs, refs = refs[:piece_count], refs[piece_count:]
    weights, gathered_ref = refs[:-1], refs[-1]
    count = piece_refs[0].shape[0]
    for n, ref in enumerate(piece_refs):
        gathered_ref[n * count : n * count + count] = ref[...]
    left_half = lax.broadcasted_iota(jnp.int32, (HALF, 128), 1) < BS
    offset = 0
    for (rows, cols), ref in zip(SHAPES, weights):
        wide = cols // BS
        for rb in range(rows // BS):
            for cb in range(0, wide, 2):
                number = offset + rb * wide + cb
                first = gathered_ref[slot_ref[number]]
                turned = pltpu.roll(first, BS, 1)
                if cb + 1 < wide:
                    second = gathered_ref[slot_ref[number + 1]]
                    top = jnp.where(left_half, first, pltpu.roll(second, BS, 1))
                    low = jnp.where(left_half, turned, second)
                else:
                    top = jnp.where(left_half, first, 0.0)
                    low = jnp.where(left_half, turned, 0.0)
                place = slice(cb * BS, cb * BS + 128)
                ref[rb * BS : rb * BS + HALF, place] = top
                ref[rb * BS + HALF : rb * BS + BS, place] = low
        offset += rows // BS * wide
    weights[3][C3:, :] = jnp.zeros((WIDE - C3, HID3), bf16)


def run_unpack(slot_of, pieces):
    slots = sum(piece.shape[0] for piece in pieces)
    return pl.pallas_call(
        functools.partial(unpack_kernel, len(pieces)),
        in_specs=[SMEM] + [VMEM_BLOCK] * len(pieces),
        out_specs=[VMEM_BLOCK] * 5,
        out_shape=[pltpu.VMEM(shape, bf16) for shape in WEIGHTS],
        scratch_shapes=[pltpu.VMEM((slots, HALF, 128), bf16)],
        compiler_params=roomy(6),
        name="unpack",
    )(slot_of, *held_in(pltpu.VMEM, *pieces))


def main_kernel(
    pairs,
    strip_count,
    slots,
    near_place,
    far_place,
    size_ref,
    inv_in,
    mix_in,
    stat_in,
    goal_ref,
    vec_two_ref,
    vec_hid_two_ref,
    vec_three_ref,
    vec_hid_three_ref,
    w1_ref,
    w2_ref,
    we_ref,
    w3_ref,
    w4_ref,
    result_ref,
    zed_out,
    dx_out,
    mean_out,
    near_ref,
    far_ref,
    flat_ref,
    zed_ref,
    hid_ref,
    u_ref,
    g_ref,
    h_ref,
    dy_ref,
    patch_ref,
    dpatch_ref,
    inv3_ref,
    e_ref,
    col3_ref,
    pool3_ref,
    mix3_ref,
    dx3_ref,
    hid3_ref,
    dhid3_ref,
    u3_ref,
    g3_ref,
    h3_ref,
    dy3_ref,
    dpre_ref,
    gw1_ref,
    gw2_ref,
    gwe_ref,
    gw3_ref,
    gw4_ref,
    acc_two,
    acc_hid_two,
    acc_three,
    acc_hid_three,
):
    pair = pl.program_id(0) if pairs > 1 else 0
    grads = [gw1_ref, gw2_ref, gwe_ref, gw3_ref, gw4_ref]
    inv_ref, mix_ref, stat_ref = (ref.at[0] for ref in (inv_in, mix_in, stat_in))
    back_ref, dx_ref = zed_out.at[0], dx_out.at[0]
    left_half = lax.broadcasted_iota(jnp.int32, (HALF, 128), 1) < BS

    def at_pair(number, act):
        if pairs == 1:
            act()
        else:
            pl.when(pair == number)(act)

    def begin():
        acc_two[...] = jnp.zeros(acc_two.shape, f32)
        acc_hid_two[...] = jnp.zeros(acc_hid_two.shape, f32)
        acc_three[...] = jnp.zeros(acc_three.shape, f32)
        acc_hid_three[...] = jnp.zeros(acc_hid_three.shape, f32)

    at_pair(0, begin)
    shape = Geometry(size_ref, pair)
    count_two, count_three, flipped = shape.count_two, shape.count_three, shape.flipped
    nothing = jnp.zeros((8, C2), f32)
    nothing3 = jnp.zeros((8, WIDE), f32)
    gain2, bias2, scale2, out_bias = (vec_two_ref[n : n + 1] for n in range(3, 7))
    embed_bias, gain3, bias3, scale3 = (vec_three_ref[n : n + 1] for n in range(4))
    gain4, bias4, scale4, out_bias3 = (vec_three_ref[n : n + 1] for n in range(4, 8))
    mean2, scaling2 = stat_ref[2], stat_ref[3]
    factor2 = scaling2 * gain2
    shift2 = bias2 - mean2 * scaling2 * gain2
    for plane in range(4):
        zed_ref[plane, 0:LINE] = jnp.zeros((LINE, C2), f32)
    col3_ref[0:LINE] = jnp.zeros((LINE, WIDE), f32)
    col3_ref[AREA + LINE : AREA + 2 * LINE] = jnp.zeros((LINE, WIDE), f32)

    def put_block(number, block):
        near_ref[near_place[number]] = block
        far_ref[far_place[number]] = block

    def pack_blocks(matrices):
        offsets = [0]
        for rows, cols in SHAPES:
            offsets.append(offsets[-1] + rows // BS * (cols // BS))
        for which in matrices:
            (rows, cols), ref = SHAPES[which], grads[which]
            wide = cols // BS
            for rb in range(rows // BS):
                for cb in range(0, wide, 2):
                    number = offsets[which] + rb * wide + cb
                    at = slice(cb * BS, cb * BS + 128)
                    top = ref[rb * BS : rb * BS + HALF, at].astype(bf16)
                    low = ref[rb * BS + HALF : rb * BS + BS, at].astype(bf16)
                    put_block(number, jnp.where(left_half, top, pltpu.roll(low, BS, 1)))
                    if cb + 1 < wide:
                        put_block(number + 1, jnp.where(left_half, pltpu.roll(top, BS, 1), low))

    def plane_rows(plane):
        return slice(plane * AREA, plane * AREA + AREA)

    def begin_plane(plane):
        low = affine(mix_ref[plane], factor2, shift2).astype(bf16)
        h_ref[plane_rows(plane)] = low
        hid_ref[plane % 2] = product(low, w1_ref[...])

    begin_plane(0)
    for plane in range(4):
        if plane < 3:
            begin_plane(plane + 1)
        for k in range(STEPS):
            rows = step_rows(k)
            flat = slice(plane * AREA + k * STEP, plane * AREA + k * STEP + STEP)
            for at in range(0, HID2, 128):
                lanes = slice(at, at + 128)
                active, slope = gelu_pair(hid_ref[plane % 2, rows, lanes] + vec_hid_two_ref[:, lanes])
                u_ref[flat, lanes] = active.astype(bf16)
                g_ref[flat, lanes] = slope.astype(bf16)
        out = product(u_ref[plane_rows(plane)], w2_ref[...]) + out_bias
        zed = jnp.where(inv_ref[plane] > 0.0, mix_ref[plane] + scale2 * out, 0.0)
        zed_ref[plane, LINE : LINE + AREA] = rounded(zed)

    def patches(k, carry):
        rows = step_rows(k)
        taps = []
        for ky in range(3):
            pr = (0 if ky == 1 else 1) * 2
            source = step_rows(k, 0 if ky == 0 else 1)
            even = zed_ref[pr, source]
            odd = zed_ref[pr + 1, source]
            taps.append((from_left(odd), even, odd))
        for ky in range(3):
            for kx in range(3):
                at = (3 * ky + kx) * C2
                tap = taps[ky][kx]
                if ky != kx:
                    tap = jnp.where(flipped, taps[kx][ky], tap)
                patch_ref[rows, at : at + C2] = tap.astype(bf16)
        return carry

    sweep(patches, 0)
    e_ref[...] = product(patch_ref[...], we_ref[...])

    def embed(k, carry):
        total, square = carry
        rows = step_rows(k)
        share = shape.share3(k)
        inv3_ref[rows] = share
        out = jnp.where(widen(share) > 0.0, e_ref[rows] + embed_bias, 0.0)
        e_ref[rows] = out
        return (total + fold(out), square + fold(out * out))

    total, square = sweep(embed, (nothing3, nothing3))
    mean3, scaling3 = norm_terms(total, square, count_three)
    factor3 = scaling3 * gain3
    shift3 = bias3 - mean3 * scaling3 * gain3

    def window_cols3(k, carry):
        rows = step_rows(k)
        normal = rounded(affine(e_ref[rows], factor3, shift3))
        masked = jnp.where(widen(inv3_ref[rows]) > 0.0, normal, 0.0)
        col3_ref[step_rows(k, 1)] = masked + from_left(masked) + from_right(masked)
        return carry

    sweep(window_cols3, 0)

    def row_windows3(k):
        return col3_ref[step_rows(k)] + col3_ref[step_rows(k, 1)] + col3_ref[step_rows(k, 2)]

    def mix3(k, carry):
        total, square = carry
        rows = step_rows(k)
        values = e_ref[rows]
        share = widen(inv3_ref[rows])
        pooled = row_windows3(k) * share - rounded(affine(values, factor3, shift3))
        pooled = jnp.where(share > 0.0, pooled, 0.0)
        mixed = values + scale3 * pooled
        pool3_ref[rows] = pooled
        mix3_ref[rows] = mixed
        return (total + fold(mixed), square + fold(mixed * mixed))

    total, square = sweep(mix3, (nothing3, nothing3))
    mean4, scaling4 = norm_terms(total, square, count_three)
    factor4 = scaling4 * gain4
    shift4 = bias4 - mean4 * scaling4 * gain4
    normal4 = (spread(scaling4, WIDE), spread(-mean4 * scaling4, WIDE))

    def prepare3(k, d_bias):
        rows = step_rows(k)
        h3_ref[rows] = affine(mix3_ref[rows], factor4, shift4).astype(bf16)
        goal = goal_ref[0, rows].astype(f32)
        goal = jnp.where(widen(inv3_ref[rows]) > 0.0, goal, 0.0)
        low_goal = (scale4 * goal).astype(bf16)
        dy3_ref[rows] = low_goal
        return d_bias + fold(low_goal.astype(f32))

    acc_three[7] += sweep(prepare3, nothing3)

    def keep(ref, value, place=slice(None)):
        if pairs == 1:
            ref[place] = value.astype(ref.dtype)
        else:

            @pl.when(pair == 0)
            def _():
                ref[place] = value

            @pl.when(pair > 0)
            def _():
                ref[place] += value

    def begin_chunk(at):
        lanes = slice(at, at + 256)
        hid3_ref[:, lanes] = product(h3_ref[...], w3_ref[:, lanes])
        dhid3_ref[:, lanes] = product_nt(dy3_ref[...], w4_ref[lanes])

    begin_chunk(0)
    for at in range(0, HID3, 256):
        if at + 256 < HID3:
            begin_chunk(at + 256)
        for lane in (at, at + 128):
            lanes = slice(lane, lane + 128)
            total = nothing
            for k in range(STEPS):
                rows = step_rows(k)
                active, slope = gelu_pair(hid3_ref[rows, lanes] + vec_hid_three_ref[:, lanes])
                u3_ref[rows, lanes] = active.astype(bf16)
                low = (slope * dhid3_ref[rows, lanes]).astype(bf16)
                g3_ref[rows, lanes] = low
                total = total + fold(low.astype(f32))
            acc_hid_three[:, lanes] += total
        lanes = slice(at, at + 256)
        out = product(u3_ref[:, lanes], w4_ref[lanes])
        d_low = product_nt(g3_ref[:, lanes], w3_ref[:, lanes])
        result_ref[0] = out if at == 0 else result_ref[0] + out
        dx3_ref[...] = d_low if at == 0 else dx3_ref[...] + d_low

    def finish3(k, carry):
        d_scale, d_shift, d_gain = carry
        rows = step_rows(k)
        valid = widen(inv3_ref[rows]) > 0.0
        mixed = mix3_ref[rows]
        out = jnp.where(valid, result_ref[0, rows] + out_bias3, 0.0)
        result_ref[0, rows] = mixed + scale4 * out
        d_scale = d_scale + fold(out * goal_ref[0, rows].astype(f32))
        d_low = dx3_ref[rows]
        normal = affine(mixed, *normal4)
        return (d_scale, d_shift + fold(d_low), d_gain + fold(d_low * normal))

    d_scale, d_shift, d_gain = sweep(finish3, (nothing3, nothing3, nothing3))
    acc_three[6] += d_scale
    acc_three[5] += d_shift
    acc_three[4] += d_gain
    mean_shift = by_image(d_shift * gain4) / count_three
    mean_gain = by_image(d_gain * gain4) / count_three
    back_gain4 = scaling4 * gain4
    back_mean4 = spread(-scaling4 * mean_shift, WIDE)
    back_normal4 = spread(scaling4 * mean_gain, WIDE)

    def unmix3(k, d_scale):
        rows = step_rows(k)
        share = widen(inv3_ref[rows])
        valid = share > 0.0
        normal = affine(mix3_ref[rows], *normal4)
        back = affine(dx3_ref[rows], back_gain4, back_mean4) - scaled(normal, back_normal4)
        d_mixed = jnp.where(valid, back + goal_ref[0, rows].astype(f32), 0.0)
        dx3_ref[rows] = d_mixed
        d_scale = d_scale + fold(pool3_ref[rows] * d_mixed)
        weighted = scale3 * d_mixed * share
        col3_ref[step_rows(k, 1)] = weighted + from_left(weighted) + from_right(weighted)
        return d_scale

    for at in range(0, HID3, 256):
        lanes = slice(at, at + 256)
        keep(gw3_ref, product_tn(h3_ref[...], g3_ref[:, lanes]), (slice(None), lanes))
    acc_three[3] += sweep(unmix3, nothing3)
    for at in range(0, HID3, 256):
        lanes = slice(at, at + 256)
        keep(gw4_ref, product_tn(u3_ref[:, lanes], dy3_ref[...]), lanes)
    normal3 = (spread(scaling3, WIDE), spread(-mean3 * scaling3, WIDE))

    def unpool3(k, carry):
        d_shift, d_gain = carry
        rows = step_rows(k)
        valid = widen(inv3_ref[rows]) > 0.0
        d_normal = jnp.where(valid, row_windows3(k) - scale3 * dx3_ref[rows], 0.0)
        pool3_ref[rows] = d_normal
        normal = affine(e_ref[rows], *normal3)
        return (d_shift + fold(d_normal), d_gain + fold(d_normal * normal))

    d_shift, d_gain = sweep(unpool3, (nothing3, nothing3))
    acc_three[2] += d_shift
    acc_three[1] += d_gain
    mean_shift = by_image(d_shift * gain3) / count_three
    mean_gain = by_image(d_gain * gain3) / count_three
    back_gain3 = scaling3 * gain3
    back_mean3 = spread(-scaling3 * mean_shift, WIDE)
    back_normal3 = spread(scaling3 * mean_gain, WIDE)

    def unnorm3(k, d_bias):
        rows = step_rows(k)
        valid = widen(inv3_ref[rows]) > 0.0
        normal = affine(e_ref[rows], *normal3)
        back = affine(pool3_ref[rows], back_gain3, back_mean3) - scaled(normal, back_normal3)
        low = jnp.where(valid, dx3_ref[rows] + back, 0.0).astype(bf16)
        dpre_ref[rows] = low
        return d_bias + fold(low.astype(f32))

    acc_three[0] += sweep(unnorm3, nothing3)
    dpatch_ref[0:AREA] = product_nt(dpre_ref[...], we_ref[...])
    dpatch_ref[AREA : AREA + LINE] = jnp.zeros((LINE, 9 * C2), f32)
    keep(gwe_ref, product_tn(patch_ref[...], dpre_ref[...]))

    def gather_back(k, carry):
        rows = step_rows(k)

        def tap(ky, kx, source):
            at = (3 * ky + kx) * C2
            value = dpatch_ref[source, at : at + C2]
            if ky != kx:
                at = (3 * kx + ky) * C2
                value = jnp.where(flipped, dpatch_ref[source, at : at + C2], value)
            return value

        sources = []
        for ky in range(3):
            source = step_rows(k, 1 if ky == 0 else 0)
            sources.append(
                (tap(ky, 1, source), tap(ky, 2, source) + from_right(tap(ky, 0, source)))
            )
        for pc in range(2):
            for pr, value in ((0, sources[1][pc]), (1, sources[2][pc] + sources[0][pc])):
                plane = pr * 2 + pc
                valid = inv_ref[plane, rows] > 0.0
                back_ref[plane, rows] = jnp.where(valid, rounded(value), 0.0)
        return carry

    sweep(gather_back, 0)

    if pairs == 1:
        pack_blocks(range(2, 5))

    normal2 = (spread(scaling2, C2), spread(-mean2 * scaling2, C2))

    def begin_back(plane):
        low_goal = (scale2 * back_ref[plane]).astype(bf16)
        dy_ref[plane_rows(plane)] = low_goal
        hid_ref[plane % 2] = product_nt(low_goal, w2_ref[...])
        return fold(low_goal.astype(f32))

    d_out_bias = begin_back(0)
    d_shift, d_gain = nothing, nothing
    sums = [nothing] * (HID2 // 128)
    new_gw1, new_gw2 = None, None
    for plane in range(4):
        if plane < 3:
            d_out_bias = d_out_bias + begin_back(plane + 1)
        for k in range(STEPS):
            rows = step_rows(k)
            part = slice(plane * AREA + k * STEP, plane * AREA + k * STEP + STEP)
            for n, at in enumerate(range(0, HID2, 128)):
                lanes = slice(at, at + 128)
                low = g_ref[part, lanes].astype(f32) * hid_ref[plane % 2, rows, lanes]
                low = low.astype(bf16)
                g_ref[part, lanes] = low
                sums[n] = sums[n] + fold(low.astype(f32))
        flat = plane_rows(plane)
        d_low = product_nt(g_ref[flat], w1_ref[...])
        dx_ref[plane] = d_low
        d_shift = d_shift + fold(d_low)
        d_gain = d_gain + fold(d_low * affine(mix_ref[plane], *normal2))
        part_gw1 = product_tn(h_ref[flat], g_ref[flat])
        part_gw2 = product_tn(dy_ref[flat], u_ref[flat])
        new_gw1 = part_gw1 if plane == 0 else new_gw1 + part_gw1
        new_gw2 = part_gw2 if plane == 0 else new_gw2 + part_gw2
    new_gw2 = new_gw2.T
    for n, value in enumerate(sums):
        acc_hid_two[:, n * 128 : n * 128 + 128] += value
    acc_two[6] += d_out_bias
    acc_two[4] += d_shift
    acc_two[3] += d_gain
    mean_out[0, 0] = spread(by_image(d_shift * gain2) / count_two, 128)
    mean_out[0, 1] = spread(by_image(d_gain * gain2) / count_two, 128)
    keep(gw1_ref, new_gw1)
    keep(gw2_ref, new_gw2)
    d_scale = fold(w2_ref[...].astype(f32) * new_gw2) + out_bias * d_out_bias
    acc_two[5] += d_scale / scale2

    def finish():
        if pairs > 1:
            pack_blocks(range(5))
        else:
            pack_blocks(range(2))

        def filler(number, carry):
            put_block(number, jnp.zeros((HALF, 128), bf16))
            return carry

        lax.fori_loop(USED, slots, filler, 0)

        flat_ref[...] = jnp.zeros(flat_ref.shape, f32)

        def put(at, total, length):
            if at % 128:
                room = jnp.zeros((8, 128), f32)
                if total.shape[1] < length + BS:
                    total = jnp.concatenate([total, room], axis=1)
                total = pltpu.roll(total, BS, 1)
            whole = jnp.sum(total, axis=0, keepdims=True)
            done = -(at % 128)
            row = at // 128
            lane = 0
            while done < length:
                first = max(0, -done)
                last = min(128, length - done)
                flat_ref[row : row + 1, first:last] = whole[:, lane + first : lane + last]
                done += 128
                lane += 128
                row += 1

        at = 3 * C2
        for n in range(3, 6):
            put(at, acc_two[n], C2)
            at += C2
        put(at, acc_hid_two[...], HID2)
        at += HID2
        put(at, acc_two[6], C2)
        at += C2
        for n in range(7):
            put(at, acc_three[n], C3)
            at += C3
        put(at, acc_hid_three[...], HID3)
        at += HID3
        put(at, acc_three[7], C3)

    at_pair(pairs - 1, finish)


def run_main(places, sizes, state, goal, vectors, weights, strip_count):
    pairs = goal.shape[0]
    slots = places[0].shape[0]
    half = slots // 2 + 1
    if pairs == 1:
        state = held_in(pltpu.VMEM, *state)
    weights = held_in(pltpu.VMEM, *weights)
    _, inv, _, mix, stat = state
    state_shapes = [STATE[1], STATE[3], STATE[4]]
    grad_kind = bf16 if pairs == 1 else f32
    wide_f32 = pltpu.VMEM((AREA, WIDE), f32)
    wide_bf16 = pltpu.VMEM((AREA, WIDE), bf16)
    scratch = [
        pltpu.VMEM((4, AREA + LINE, C2), f32),
        pltpu.VMEM((2, AREA, HID2), f32),
        pltpu.VMEM((4 * AREA, HID2), bf16),
        pltpu.VMEM((4 * AREA, HID2), bf16),
        pltpu.VMEM((4 * AREA, C2), bf16),
        pltpu.VMEM((4 * AREA, C2), bf16),
        pltpu.VMEM((AREA, 9 * C2), bf16),
        pltpu.VMEM((AREA + LINE, 9 * C2), f32),
        pltpu.VMEM((AREA, 128), f32),
        wide_f32,
        pltpu.VMEM((AREA + 2 * LINE, WIDE), f32),
        wide_f32,
        wide_f32,
        wide_f32,
        pltpu.VMEM((AREA, HID3), f32),
        pltpu.VMEM((AREA, HID3), f32),
        pltpu.VMEM((AREA, HID3), bf16),
        pltpu.VMEM((AREA, HID3), bf16),
        wide_bf16,
        wide_bf16,
        wide_bf16,
        pltpu.VMEM((C2, HID2), grad_kind),
        pltpu.VMEM((HID2, C2), grad_kind),
        pltpu.VMEM((9 * C2, WIDE), grad_kind),
        pltpu.VMEM((WIDE, HID3), grad_kind),
        pltpu.VMEM((HID3, WIDE), grad_kind),
        pltpu.VMEM((7, 8, C2), f32),
        pltpu.VMEM((8, HID2), f32),
        pltpu.VMEM((8, 8, WIDE), f32),
        pltpu.VMEM((8, HID3), f32),
    ]
    out_shapes = [(half, HALF, 128), (half, HALF, 128), (VEC_BLOCKS * HALF, 128)]
    make = pltpu.VMEM if pairs == 1 else jax.ShapeDtypeStruct
    return pl.pallas_call(
        functools.partial(main_kernel, pairs, strip_count, slots),
        grid=() if pairs == 1 else (pairs,),
        in_specs=[SMEM] * 3
        + pair_specs(pairs, state_shapes + [goal.shape[1:]], pl.Buffered(1))
        + whole_specs(pairs, [vector.shape for vector in vectors])
        + [VMEM_BLOCK] * 5,
        out_specs=pair_specs(pairs, [(AREA, WIDE)] + BACK) + whole_specs(pairs, out_shapes),
        out_shape=pair_arrays(pairs, [(AREA, WIDE)] + BACK, [f32] * 4)
        + [make(shape, kind) for shape, kind in zip(out_shapes, (bf16, bf16, f32))],
        scratch_shapes=scratch,
        compiler_params=pltpu.CompilerParams(
            vmem_limit_bytes=(40 if pairs == 1 else 56) * 1024 * 1024,
            fuse_transposed_lhs_in_matmul=True,
        ),
        name="blocks",
    )(*places, sizes, inv, mix, stat, goal, *vectors, *weights)


def exit_kernel(
    pairs,
    strip_count,
    size_ref,
    x_in,
    inv_in,
    pool_in,
    mix_in,
    stat_in,
    zed_in,
    dx_in,
    mean_in,
    flat_ref,
    vec_two_ref,
    payload_hbm,
    vector_ref,
    payload_ref,
    image_ref,
    col_ref,
    dx_ref,
    back_ref,
    acc_ref,
    sem,
):
    pair = pl.program_id(0) if pairs > 1 else 0
    x_ref, inv_ref, pool_ref, mix_ref, stat_ref, zed_ref, low_ref, mean_ref = (
        ref.at[0] for ref in (x_in, inv_in, pool_in, mix_in, stat_in, zed_in, dx_in, mean_in)
    )
    shape = Geometry(size_ref, pair)
    count_two = shape.count_two
    gain1, bias1, scale1, gain2 = (vec_two_ref[n : n + 1] for n in range(4))
    mean1, scaling1, mean2, scaling2 = (stat_ref[n] for n in range(4))
    normal2 = (scaling2, -mean2 * scaling2)
    clear_edges(col_ref)
    nothing = jnp.zeros((8, C2), f32)
    back_gain2 = scaling2 * gain2
    back_mean2 = -scaling2 * mean_ref[0]
    back_normal2 = scaling2 * mean_ref[1]

    if pairs > 1:

        @pl.when(pair == 0)
        def _():
            acc_ref[...] = jnp.zeros(acc_ref.shape, f32)

    def add_up(n, total):
        acc_ref[n] = total if pairs == 1 else acc_ref[n] + total

    def unmix(k, d_scale):
        rows = step_rows(k)
        for pr in range(2):
            weighted = []
            for pc in range(2):
                plane = pr * 2 + pc
                share = inv_ref[plane, rows]
                normal = affine(mix_ref[plane, rows], *normal2)
                back = affine(low_ref[plane, rows], back_gain2, back_mean2)
                back = back - scaled(normal, back_normal2)
                d_mixed = jnp.where(share > 0.0, zed_ref[plane, rows] + back, 0.0)
                dx_ref[plane, rows] = d_mixed
                d_scale = d_scale + fold(pool_ref[plane, rows] * d_mixed)
                weighted.append(scale1 * d_mixed * share)
            put_col_windows(col_ref, pr, k, *weighted)
        return d_scale

    add_up(2, sweep(unmix, nothing))
    normal1 = (spread(scaling1, C2), spread(-mean1 * scaling1, C2))

    def unpool(k, carry):
        d_shift, d_gain = carry
        rows = step_rows(k)
        for pc in range(2):
            windows = row_windows(col_ref, pc, k)
            for pr in range(2):
                plane = pr * 2 + pc
                valid = inv_ref[plane, rows] > 0.0
                d_normal = windows[pr] - scale1 * dx_ref[plane, rows]
                d_normal = jnp.where(valid, d_normal, 0.0)
                back_ref[plane, rows] = d_normal
                normal = affine(x_ref[plane, rows], *normal1)
                d_shift = d_shift + fold(d_normal)
                d_gain = d_gain + fold(d_normal * normal)
        return (d_shift, d_gain)

    d_shift, d_gain = sweep(unpool, (nothing, nothing))
    add_up(1, d_shift)
    add_up(0, d_gain)
    mean_shift = by_image(d_shift * gain1) / count_two
    mean_gain = by_image(d_gain * gain1) / count_two
    back_gain1 = scaling1 * gain1
    back_mean1 = spread(-scaling1 * mean_shift, C2)
    back_normal1 = spread(scaling1 * mean_gain, C2)

    def unnorm(k, carry):
        rows = step_rows(k)
        for plane in range(4):
            normal = affine(x_ref[plane, rows], *normal1)
            back = affine(back_ref[plane, rows], back_gain1, back_mean1)
            back = back - scaled(normal, back_normal1)
            valid = inv_ref[plane, rows] > 0.0
            dx_ref[plane, rows] = jnp.where(valid, dx_ref[plane, rows] + back, 0.0)
        return carry

    sweep(unnorm, 0)

    def give_back(image, plane, line_place, there):
        image_ref[image, there] = dx_ref[plane, line_place]

    image_ref[...] = jnp.zeros(image_ref.shape, f32)
    each_image(size_ref, pair, give_back)

    def from_rows(within, carry):
        for spot in range(2 * STRIPS):
            image, strip = spot // STRIPS, spot % STRIPS
            start = pl.multiple_of((strip * SR + within) * LINE, LINE)
            target = strip_place(pair, spot, strip_count)
            payload_ref[target, within] = image_ref[image, pl.ds(start, CW)].astype(bf16)
        return carry

    lax.fori_loop(0, SR, from_rows, 0)

    def finish():
        copy = pltpu.make_async_copy(payload_ref, payload_hbm, sem)
        copy.start()
        vector_ref[...] = flat_ref[...]
        for n in range(3):
            vector_ref[n : n + 1] = jnp.sum(acc_ref[n], axis=0, keepdims=True)
        copy.wait()

    if pairs == 1:
        finish()
    else:
        pl.when(pair == pairs - 1)(finish)


def run_exit(sizes, state, back, flat, vec_two, strip_count):
    pairs = strip_count // 8
    payload = (strip_count, SR, CW, C2)
    make = pltpu.VMEM if pairs == 1 else jax.ShapeDtypeStruct
    plane_f32 = pltpu.VMEM((4, AREA, C2), f32)
    arrays = [*state, *back]
    if pairs == 1:
        arrays = held_in(pltpu.VMEM, *arrays)
    return pl.pallas_call(
        functools.partial(exit_kernel, pairs, strip_count),
        grid=() if pairs == 1 else (pairs,),
        in_specs=[SMEM]
        + pair_specs(pairs, STATE + BACK, pl.Buffered(1))
        + whole_specs(pairs, [flat.shape, vec_two.shape]),
        out_specs=[HBM] + whole_specs(pairs, [flat.shape]),
        out_shape=[pltpu.HBM(payload, bf16), make(flat.shape, f32)],
        scratch_shapes=[
            pltpu.VMEM(payload, bf16),
            pltpu.VMEM((2, CH * LINE, C2), f32),
            pltpu.VMEM((4, AREA + 2 * LINE, C2), f32),
            plane_f32,
            plane_f32,
            pltpu.VMEM((3, 8, C2), f32),
            pltpu.SemaphoreType.DMA,
        ],
        compiler_params=roomy(8 if pairs == 1 else 40),
        name="exit",
    )(sizes, *arrays, flat, vec_two)


def pack_kernel(master_ref, dense_ref):
    values = master_ref[...]
    dense_ref[...] = jnp.concatenate([values[:, :HALF], values[:, HALF:]], axis=2).astype(bf16)


def pack(master):
    owned = master.shape[0]
    return pl.pallas_call(
        pack_kernel,
        out_shape=jax.ShapeDtypeStruct((owned, HALF, 2 * BS), bf16),
        name="pack",
    )(master)


def fold_pair_kernel(near_ref, got_ref, own_ref, *part_refs):
    share = own_ref.shape[0]

    def one(n, carry):
        for k in range(len(part_refs) + 1):
            total = near_ref[k * share + n].astype(f32) + got_ref[k * share + n].astype(f32)
            if k == 0:
                own_ref[n] = total
            else:
                part_refs[k - 1][n] = total.astype(bf16)
        return carry

    lax.fori_loop(0, share, one, 0, unroll=4)


def fold_pair(near, got, groups):
    shape = ((near.shape[0] - 1) // groups,) + near.shape[1:]
    return pl.pallas_call(
        fold_pair_kernel,
        in_specs=[VMEM_BLOCK] * 2,
        out_specs=[VMEM_BLOCK] * groups,
        out_shape=[pltpu.VMEM(shape, f32)] + [pltpu.VMEM(shape, bf16)] * (groups - 1),
        compiler_params=roomy(4),
        name="fold_pair",
    )(*held_in(pltpu.VMEM, near, got))


def fold_tile_kernel(pieces, spot_ref, *refs):
    piece_refs, refs = refs[:pieces], refs[pieces:]
    vector_refs, refs = refs[:pieces], refs[pieces:]
    out_refs, sum_ref = refs[:-1], refs[-1]
    groups = len(out_refs)
    share = out_refs[0].shape[0]
    owned = piece_refs[0].shape[0]
    total = vector_refs[0][...]
    for ref in vector_refs[1:]:
        total = total + ref[...]
    for n in range(sum_ref.shape[0]):
        sum_ref[n] = jnp.zeros((HALF, 128), f32)
    for n in range(VEC_BLOCKS):
        sum_ref[n] = total[n * HALF : (n + 1) * HALF]

    def one(n, carry):
        for k, out_ref in enumerate(out_refs):
            number = lax.rem(spot_ref[0] + k, groups) * share + n
            block = jnp.minimum(number, owned - 1)
            total = piece_refs[0][block].astype(f32)
            for ref in piece_refs[1:]:
                total = total + ref[block].astype(f32)
            rest = sum_ref[jnp.maximum(number - owned, 0)]
            out_ref[n] = jnp.where(number < owned, total, rest).astype(out_ref.dtype)
        return carry

    lax.fori_loop(0, share, one, 0, unroll=share <= 16)


def fold_tile(spot, pieces, vectors, extra, groups):
    shape = ((pieces[0].shape[0] + extra) // groups,) + pieces[0].shape[1:]
    return pl.pallas_call(
        functools.partial(fold_tile_kernel, len(pieces)),
        in_specs=[SMEM] + [VMEM_BLOCK] * (len(pieces) + len(vectors)),
        out_specs=[VMEM_BLOCK] * groups,
        out_shape=[pltpu.VMEM(shape, f32)] + [pltpu.VMEM(shape, bf16)] * (groups - 1),
        scratch_shapes=[pltpu.VMEM((extra, HALF, 128), f32)],
        compiler_params=roomy(8),
        name="fold_tile",
    )(spot, *held_in(pltpu.VMEM, *pieces, *vectors))


def fold_batch_kernel(owned, vector_weight, spot_ref, *refs):
    part_refs, (total_ref, norm_ref) = refs[:-2], refs[-2:]
    share = total_ref.shape[0]
    square = jnp.zeros((8, 128), f32)
    for n in range(share):
        total = part_refs[0][n].astype(f32)
        for ref in part_refs[1:]:
            total = total + ref[n].astype(f32)
        total_ref[n] = total.astype(bf16)
        weight = jnp.where(spot_ref[0] * share + n < owned, 1.0, vector_weight)
        square = square + weight * fold(total * total)
    square = jnp.sum(jnp.sum(square, axis=1, keepdims=True), axis=0, keepdims=True)
    norm_ref[...] = jnp.broadcast_to(square[None], norm_ref.shape)


def fold_batch(spot, parts, owned, tile_count):
    count = tile_count * len(parts)
    return pl.pallas_call(
        functools.partial(fold_batch_kernel, owned, 1.0 / tile_count),
        in_specs=[SMEM] + [VMEM_BLOCK] * len(parts),
        out_specs=[VMEM_BLOCK] * 2,
        out_shape=[pltpu.VMEM(parts[0].shape, bf16), pltpu.VMEM((count, 1, 128), f32)],
        name="fold_batch",
    )(spot, *held_in(pltpu.VMEM, *parts))


def update_kernel(owned, groups, spot_ref, norm_ref, *refs):
    quarters, refs = refs[:groups], refs[groups:]
    stat_hbm, out_hbm, (vector_ref, clip_ref), refs = refs[:5], refs[5:10], refs[10:12], refs[12:]
    stat_refs, out_refs, (in_sem, out_sem) = refs[:5], refs[5:10], refs[10:]
    master_ref, left_stat_ref, right_stat_ref, left_root_ref, right_root_ref = stat_refs
    grad_ref, left_ref, right_ref, new_ref, copy_ref = out_refs
    share = quarters[0].shape[0]
    spans = spans_of(owned)

    def copies_of(sources, targets, sems):
        return [
            [
                pltpu.make_async_copy(
                    source.at[pl.ds(*span)], target.at[pl.ds(*span)], sems.at[5 * n + k]
                )
                for k, (source, target) in enumerate(zip(sources, targets))
            ]
            for n, span in enumerate(spans)
        ]

    copies_in = copies_of(stat_hbm, stat_refs, in_sem)
    copies_out = copies_of(out_refs, out_hbm, out_sem)
    for copies in copies_in:
        for copy in copies:
            copy.start()
    norm = jnp.sqrt(jnp.sum(norm_ref[...], axis=0))
    factor = jnp.minimum(1.0, clip_limit / norm)
    left_half = lax.broadcasted_iota(jnp.int32, (HALF, 128), 1) < BS

    def summed(number):
        source = number // share
        local = number - source * share
        turn = lax.rem(spot_ref[0] - source + groups, groups)
        value = quarters[0][local].astype(f32)
        for k in range(1, groups):
            value = jnp.where(turn == k, quarters[k][local].astype(f32), value)
        return value * factor

    def side_by_side(first, count):
        sides = []
        for n in range(first, first + count, 2):
            dense = summed(n)
            turned = pltpu.roll(dense, BS, 1)
            if n + 1 < first + count:
                second = summed(n + 1)
                top = jnp.where(left_half, dense, pltpu.roll(second, BS, 1))
                low = jnp.where(left_half, turned, second)
                side = jnp.concatenate([top, low], axis=0)
                grad_ref[n + 1] = pltpu.roll(side, BS, 1)[:, :BS]
            else:
                side = jnp.concatenate([dense, turned], axis=0)[:, :BS]
            grad_ref[n] = side[:, :BS]
            sides.append(side.astype(bf16))
        return jnp.concatenate(sides, axis=1)

    def diagonal_of(count):
        order = (count * BS, count * BS)
        return lax.broadcasted_iota(jnp.int32, order, 0) // BS == (
            lax.broadcasted_iota(jnp.int32, order, 1) // BS
        )

    clip_ref[...] = norm
    for n in range(vector_ref.shape[0]):
        vector_ref[n] = summed(owned + n)
    for (first, length), arriving, leaving in zip(spans, copies_in, copies_out):
        parts = [(n, min(4, first + length - n)) for n in range(first, first + length, 4)]
        wides = [side_by_side(*part) for part in parts]
        tall = [
            jnp.where(diagonal_of(count), jnp.concatenate([wide] * count, axis=0), 0.0)
            for (_, count), wide in zip(parts, wides)
        ]
        lefts = [product_nt(one, wide) for one, wide in zip(tall, wides)]
        rights = [product_tn(wide, wide) for wide in wides]
        for copy in arriving:
            copy.wait()
        stepped = []
        for (start, count), wide in zip(parts, wides):
            roots = left_root_ref[pl.ds(start, count)].reshape(count * BS, BS).astype(bf16)
            stepped.append(product(roots, wide))
        for (start, count), left, right in zip(parts, lefts, rights):
            here = pl.ds(start, count)
            left_ref[here] = 0.5 * left_stat_ref[here] + 0.5 * left.reshape(count, BS, BS)
            for n in range(count):
                at = n // 2 * 128
                block = right[n * BS : n * BS + BS, at : min(at + 128, count * BS)]
                if n % 2:
                    block = pltpu.roll(block, BS, 1)
                right_ref[start + n] = 0.5 * right_stat_ref[start + n] + 0.5 * block[:, :BS]
        for (start, count), value in zip(parts, stepped):
            here = pl.ds(start, count)
            value = jnp.where(diagonal_of(count), value, 0.0).astype(bf16)
            roots = right_root_ref[here].reshape(count * BS, BS).astype(bf16)
            value = product(value, roots).reshape(count, BS, BS)
            new = master_ref[here] - rate_matrix * value
            new_ref[here] = new
            copy_ref[here] = new.astype(bf16)
        for copy in leaving:
            copy.start()
    for leaving in copies_out:
        for copy in leaving:
            copy.wait()


def spans_of(owned):
    spans = []
    first = 0
    while first < owned:
        length = min(8 if first == 0 else 12, owned - first)
        spans.append((first, length))
        first += length
    return spans


def update(spot, norm, quarters, extra, *stats):
    shape = stats[0].shape
    groups = len(quarters)
    types = [f32] * 4 + [bf16]
    steps = len(spans_of(shape[0]))
    return pl.pallas_call(
        functools.partial(update_kernel, shape[0], groups),
        in_specs=[SMEM] + [VMEM_BLOCK] * (groups + 1) + [HBM] * 5,
        out_specs=[HBM] * 5 + [VMEM_BLOCK] * 2,
        out_shape=[pltpu.HBM(shape, kind) for kind in types]
        + [
            jax.ShapeDtypeStruct((extra, HALF, 128), f32),
            jax.ShapeDtypeStruct((1, 128), f32),
        ],
        scratch_shapes=[pltpu.VMEM(shape, f32)] * 5
        + [pltpu.VMEM(shape, kind) for kind in types]
        + [
            pltpu.SemaphoreType.DMA((5 * steps,)),
            pltpu.SemaphoreType.DMA((5 * steps,)),
        ],
        compiler_params=roomy(20),
        name="update",
    )(spot, *held_in(pltpu.VMEM, norm, *quarters), *held_in(pltpu.HBM, *stats))


def share_out(pieces, axis):
    return lax.all_to_all(pieces, axis, split_axis=0, concat_axis=0, tiled=True)


def swap(piece, distance):
    count = lax.axis_size("tile")
    return lax.ppermute(piece, "tile", [(i, i ^ distance) for i in range(count)])


def on_device(
    pixels,
    buckets,
    slot_owner_table,
    out_grad,
    master,
    left_stat,
    right_stat,
    left_root,
    right_root,
    vectors,
    moment,
):
    tile_count = lax.axis_size("tile")
    tile_place = lax.axis_index("tile")
    slot_count = pixels.shape[2]
    group_count = tile_count // STRIPS
    pairs = group_count // 2
    owned = master.shape[0]
    slots = owned * tile_count
    batch_count = lax.axis_size("batch")
    spot = lax.axis_index("batch").astype(jnp.int32).reshape(1)
    extra = extra_of(owned, batch_count)
    strips = share_out(pixels.reshape((tile_count,) + pixels.shape[3:]), "tile")
    dense = pack(master)
    paired = tile_count <= 8
    if paired:
        mine = [dense] + [swap(dense, 2 * k) for k in range(1, tile_count // 2)]
        pieces = mine + [swap(piece, 1) for piece in mine]
    else:
        pieces = [lax.all_gather(dense, "tile", axis=0, tiled=True)]

    numbers = jnp.arange(slots, dtype=jnp.int32)
    slot_of = jnp.sum(
        jnp.where(slot_owner_table[None, :] == numbers[:, None], numbers[None, :], 0), axis=1
    )
    owner = slot_of // owned
    within = slot_of - owner * owned
    place_of = slot_of
    if paired:
        apart = owner ^ tile_place
        apart = (apart & 1) * (tile_count // 2) + (apart >> 1)
        slot_of = place_of = within + owned * apart
    half = slots // 2
    near_place = jnp.where(place_of < half, place_of, half)
    far_place = jnp.where(place_of < half, half, place_of - half)
    image_ids = lax.dynamic_index_in_dim(
        buckets.reshape(group_count, slot_count), tile_place, 1, keepdims=False
    )
    turned = image_ids >= 2
    heights = jnp.where(image_ids == 0, 5 * CH // 9, jnp.where(image_ids == 1, 7 * CH // 9, CH))
    breadths = jnp.where(image_ids == 0, CW, jnp.where(image_ids == 1, 7 * CW // 9, 5 * CW // 9))
    sizes = jnp.stack(
        [
            jnp.where(turned, breadths, heights),
            jnp.where(turned, heights, breadths),
            turned,
        ],
        axis=1,
    )
    sizes = sizes.reshape(-1).astype(jnp.int32)

    two = 6 * C2 + HID2 + C2
    vec_two = jnp.concatenate([vectors[: 6 * C2], vectors[6 * C2 + HID2 : two]]).reshape(7, C2)
    vec_hid_two = vectors[6 * C2 : 6 * C2 + HID2].reshape(1, HID2)
    wide_end = two + 7 * C3
    vec_three = jnp.concatenate([vectors[two:wide_end], vectors[wide_end + HID3 :]])
    vec_three = jnp.pad(vec_three.reshape(8, C3), ((0, 0), (0, WIDE - C3)))
    vec_hid_three = vectors[wide_end : wide_end + HID3].reshape(1, HID3)

    flips = turned.reshape(-1, 1, 1, 1)
    goal = out_grad.reshape(2 * pairs, H3, W3, C3)
    goal = jnp.where(flips, goal.transpose(0, 2, 1, 3), goal)[:, :LINES]
    goal = goal.reshape(pairs, 2, LINES, W3, C3).transpose(0, 2, 3, 1, 4)
    goal = goal.reshape(pairs, LINES, 2 * W3, C3)
    goal = jnp.pad(goal, ((0, 0), (0, 0), (0, LINE - 2 * W3), (0, WIDE - C3)))
    goal = goal.reshape(pairs, AREA, WIDE)

    weights = run_unpack(slot_of, pieces)
    state = run_entry(sizes, strips, vec_two)
    result, *back, near, far, flat = run_main(
        (near_place, far_place),
        sizes,
        state,
        goal,
        (vec_two, vec_hid_two, vec_three, vec_hid_three),
        weights,
        tile_count,
    )
    pixel_back, vector = run_exit(sizes, state, back, flat, vec_two, tile_count)
    if paired:
        own, *parts = fold_pair(near, swap(far, 1), tile_count // 2)
        pieces = [own] + [swap(part, 2 * k + 2) for k, part in enumerate(parts)]
        vector, _ = lax.optimization_barrier((vector, parts[0]))
        vector = vector + swap(vector, 1)
        vectors_in = [vector] + [swap(vector, 2 * k) for k in range(1, tile_count // 2)]
    else:
        outgoing = jnp.concatenate([near[:half], far[:half]], axis=0)
        pieces = list(share_out(outgoing.reshape(tile_count, owned, HALF, 128), "tile"))
        vectors_in = list(lax.all_gather(vector, "tile"))
    result, pieces[1] = lax.optimization_barrier((result, pieces[1]))
    result = result.reshape(pairs, LINES, LINE, WIDE)[:, :, : 2 * W3, :C3]
    result = result.reshape(pairs, LINES, W3, 2, C3).transpose(0, 3, 1, 2, 4)
    result = result.reshape(2 * pairs, LINES, W3, C3)
    result = jnp.pad(result, ((0, 0), (0, H3 - LINES), (0, 0), (0, 0)))
    result = jnp.where(flips, result.transpose(0, 2, 1, 3), result)
    result = result.reshape(1, 1, 2 * pairs, H3, W3, 1, C3)
    result, vectors_in[0] = lax.optimization_barrier((result, vectors_in[0]))
    result = result.transpose(0, 1, 2, 5, 3, 4, 6).reshape(out_grad.shape)
    own, *parts = fold_tile(spot, pieces, vectors_in, extra, batch_count)
    pixel_back, parts[0] = lax.optimization_barrier((pixel_back, parts[0]))
    returned = share_out(pixel_back, "tile")
    parts = [
        lax.ppermute(part, "batch", [(i, (i + k + 1) % batch_count) for i in range(batch_count)])
        for k, part in enumerate(parts)
    ]
    quarter, norm = fold_batch(spot, [own] + parts, owned, tile_count)
    quarters = [quarter] + [
        lax.ppermute(quarter, "batch", [(i, (i + k) % batch_count) for i in range(batch_count)])
        for k in range(1, batch_count)
    ]
    returned, norm = lax.optimization_barrier((returned, norm))
    norm = share_out(norm, ("batch", "tile"))
    returned = returned.astype(f32).transpose(1, 2, 0, 3)
    returned, quarters[-1] = lax.optimization_barrier((returned, quarters[-1]))
    returned = returned.transpose(2, 0, 1, 3).reshape(pixels.shape)
    block_grad, left_new, right_new, master_new, weight_copy, whole_vector, clip = update(
        spot, norm, quarters, extra, master, left_stat, right_stat, left_root, right_root
    )
    clip_norm = clip[0, 0]
    share = vectors.shape[0] // tile_count
    whole_vector = whole_vector.reshape(-1)
    vec_grad = lax.dynamic_slice_in_dim(whole_vector, tile_place * share, share, 0)
    vec_moment = moment + vec_grad * vec_grad
    own_vectors = lax.dynamic_slice_in_dim(vectors, tile_place * share, share, 0)
    vec_new = own_vectors - rate_vector * vec_grad / (jnp.sqrt(vec_moment) + eps_adagrad)
    return (
        result,
        returned,
        clip_norm,
        block_grad,
        left_new,
        right_new,
        master_new,
        weight_copy,
        vec_grad,
        vec_moment,
        vec_new,
    )


def solution(mesh):
    placed = (
        P("batch", "tile", None, None, None, None),
        P("batch"),
        P(),
        P("batch", "tile", None, None, None, None, None),
        P("tile", None, None),
        P("tile", None, None),
        P("tile", None, None),
        P("tile", None, None),
        P("tile", None, None),
        P(),
        P("tile"),
    )
    return jax.shard_map(
        on_device,
        mesh=mesh,
        in_specs=placed,
        out_specs=(
            P("batch", "tile", None, None, None, None, None),
            P("batch", "tile", None, None, None, None),
            P(),
            P("tile", None, None),
            P("tile", None, None),
            P("tile", None, None),
            P("tile", None, None),
            P("tile", None, None),
            P("tile"),
            P("tile"),
            P("tile"),
        ),
        check_vma=False,
    )
```

```python
import functools

import jax
import jax.numpy as jnp
from jax import lax
from jax.experimental import pallas as pl
from jax.experimental.pallas import tpu as pltpu
from jax.sharding import PartitionSpec as P

C2 = 128
HID2 = 512
C3 = 320
HID3 = 1280
CH = 36
CW = 36
STRIPS = 4
BS = 64
SR = CH // STRIPS
H3 = CH // 2
W3 = CW // 2
LONG = 7 * CH // 9
LINES = LONG // 2
WIDE = 384
LINE = 40
AREA = LINES * LINE
STEP = 2 * LINE
STEPS = AREA // STEP
HALF = BS // 2

eps_norm = 1e-05
clip_limit = 1.0
rate_matrix = 0.3
rate_vector = 0.3
eps_adagrad = 1e-08
f32 = jnp.float32
bf16 = jnp.bfloat16

SHAPES = [(C2, HID2), (HID2, C2), (9 * C2, C3), (C3, HID3), (HID3, C3)]
USED = sum(rows // BS * (cols // BS) for rows, cols in SHAPES)
VEC_ROWS = (6 * C2 + HID2 + C2 + C3 + 6 * C3 + HID3 + C3) // 128


VEC_BLOCKS = -(-VEC_ROWS // HALF)


def extra_of(owned, groups):
    return VEC_BLOCKS + -(owned + VEC_BLOCKS) % groups


def product(left, right):
    return jnp.dot(left, right, preferred_element_type=f32)


def product_nt(left, right):
    return lax.dot_general(left, right, (((1,), (1,)), ((), ())), preferred_element_type=f32)


def product_tn(left, right):
    return lax.dot_general(left, right, (((0,), (0,)), ((), ())), preferred_element_type=f32)


def gelu_pair(values):
    bell = jnp.exp2(values * values * (-0.5 * 1.4426950408889634))
    step = pl.reciprocal(1.0 + (0.3275911 * 0.7071067811865476) * jnp.abs(values), approx=True)
    tail = step * (
        0.5 * 0.254829592
        + step
        * (
            0.5 * -0.284496736
            + step
            * (0.5 * 1.421413741 + step * (0.5 * -1.453152027 + step * (0.5 * 1.061405429)))
        )
    )
    tail = tail * bell
    share = jnp.where(values >= 0.0, 1.0 - tail, tail)
    return (values * share, share + values * (bell * 0.3989422804014327))


def fold(values):
    chans = values.shape[-1]
    return jnp.sum(values.reshape(-1, 8, chans), axis=0)


def by_image(total):
    total = total + pltpu.roll(total, 4, 0)
    total = total + pltpu.roll(total, 2, 0)
    return jnp.sum(total, axis=1, keepdims=True)


def line(pattern):
    return jnp.concatenate([pattern] * (LINE // 8), axis=0)


def spread(pattern, chans):
    return jnp.broadcast_to(pattern, (8, chans))


def affine(values, factor, shift):
    tiles = values.reshape(-1, 8, values.shape[-1])
    return (tiles * factor + shift).reshape(values.shape)


def scaled(values, factor):
    tiles = values.reshape(-1, 8, values.shape[-1])
    return (tiles * factor).reshape(values.shape)


def from_left(values):
    return pltpu.roll(values, 2, 0)


def from_right(values):
    return pltpu.roll(values, values.shape[0] - 2, 0)


def rounded(values):
    return values.astype(bf16).astype(f32)


def widen(values):
    return jnp.concatenate([values] * (WIDE // 128), axis=-1)


def norm_terms(total, square, count):
    mean = by_image(total) / count
    scaling = lax.rsqrt(by_image(square) / count - mean * mean + eps_norm)
    return (mean, scaling)


def sweep(visit, start):
    return lax.fori_loop(0, STEPS, visit, start, unroll=True)


def step_rows(k, lines=0):
    start = k * STEP + lines * LINE
    return pl.ds(start if isinstance(k, int) else pl.multiple_of(start, LINE), STEP)


def held_in(space, *arrays):
    return [pltpu.with_memory_space_constraint(array, space) for array in arrays]


VMEM_BLOCK = pl.BlockSpec(memory_space=pltpu.VMEM)
HBM = pl.BlockSpec(memory_space=pltpu.HBM)
SMEM = pl.BlockSpec(memory_space=pltpu.SMEM)


def roomy(mebibytes):
    return pltpu.CompilerParams(vmem_limit_bytes=mebibytes * 1024 * 1024)


class Geometry:
    def __init__(self, size_ref, pair):
        parity = lax.broadcasted_iota(jnp.int32, (8, 128), 0) % 2
        high, broad, turned = (
            jnp.where(parity == 0, size_ref[pair * 6 + n], size_ref[pair * 6 + 3 + n])
            for n in range(3)
        )
        self.high = high
        self.count_two = (high * broad * C2).astype(f32)[:, :1]
        self.high3 = (high + 1) // 2
        broad3 = (broad + 1) // 2
        self.count_three = (self.high3 * broad3 * C3).astype(f32)[:, :1]
        place = lax.broadcasted_iota(jnp.int32, (LINE, 128), 0) // 2
        inside = lax.broadcasted_iota(jnp.int32, (LINE, 128), 0) < 2 * W3
        self.reach = []
        self.col_share = []
        for pc in range(2):
            column = 2 * place + pc
            self.reach.append(jnp.where(inside & (column < line(broad)), line(high), 0))
            edge = (column == 0) | (column == line(broad) - 1)
            self.col_share.append(jnp.where(edge, 0.5, 1.0 / 3.0))
        self.reach3 = jnp.where(inside & (place < line(broad3)), line(self.high3), 0)
        edge3 = (place == 0) | (place == line(broad3) - 1)
        self.col_share3 = jnp.where(edge3, 0.5, 1.0 / 3.0)
        self.flipped = jnp.concatenate([turned] * (STEP // 8), axis=0) > 0

    def share(self, plane, k):
        pr, pc = plane // 2, plane % 2
        return self.lines(4 * k + pr, 2, self.reach[pc], self.col_share[pc], self.high)

    def share3(self, k):
        return self.lines(2 * k, 1, self.reach3, self.col_share3, self.high3)

    def lines(self, row, stride, reach, col_share, height):
        parts = []
        for n in range(2):
            here = row + stride * n
            row_share = jnp.where((here == 0) | (here == height - 1), 0.5, 1.0 / 3.0)
            parts.append(jnp.where(here < reach, line(row_share) * col_share, 0.0))
        return jnp.concatenate(parts, axis=0)


def strip_place(pair, spot, strip_count):
    return lax.rem(pair * 8 + strip_count - 2 + spot, strip_count)


def each_image(size_ref, pair, visit):
    for image in range(2):
        way = size_ref[pair * 6 + 3 * image + 2]
        for flat in (True, False):

            @pl.when(way == (0 if flat else 1))
            def _():
                def one(r, carry):
                    for pr in range(2):
                        for pc in range(2):
                            line_place = pl.ds(r * LINE + image, W3, stride=2)
                            if flat:
                                there = pl.ds((2 * r + pr) * LINE + pc, W3, stride=2)
                            else:
                                there = pl.ds(pc * LINE + 2 * r + pr, W3, stride=2 * LINE)
                            visit(image, pr * 2 + pc, line_place, there)
                    return carry

                lax.fori_loop(0, LINES, one, 0)


def row_windows(col_ref, pc, k):
    both = col_ref[pc, step_rows(k, 1)] + col_ref[2 + pc, step_rows(k, 1)]
    return (both + col_ref[2 + pc, step_rows(k)], both + col_ref[pc, step_rows(k, 2)])


def put_col_windows(col_ref, pr, k, even, odd):
    both = even + odd
    col_ref[pr * 2, step_rows(k, 1)] = both + from_left(odd)
    col_ref[pr * 2 + 1, step_rows(k, 1)] = both + from_right(even)


def clear_edges(col_ref):
    zero_line = jnp.zeros((LINE, C2), f32)
    for plane in range(4):
        col_ref[plane, 0:LINE] = zero_line
        col_ref[plane, AREA + LINE : AREA + 2 * LINE] = zero_line


def entry_kernel(
    pairs,
    strip_count,
    size_ref,
    strips_ref,
    vec_two_ref,
    x_out,
    inv_out,
    pool_out,
    mix_out,
    stat_out,
    image_ref,
    col_ref,
):
    pair = pl.program_id(0) if pairs > 1 else 0
    x_ref, inv_ref, pool_ref, mix_ref = (ref.at[0] for ref in (x_out, inv_out, pool_out, mix_out))
    shape = Geometry(size_ref, pair)
    gain1, bias1, scale1 = (vec_two_ref[n : n + 1] for n in range(3))
    clear_edges(col_ref)

    def to_rows(within, carry):
        for spot in range(2 * STRIPS):
            image, strip = spot // STRIPS, spot % STRIPS
            start = pl.multiple_of((strip * SR + within) * LINE, LINE)
            source = strip_place(pair, spot, strip_count)
            image_ref[image, pl.ds(start, CW)] = strips_ref[source, within].astype(f32)
        return carry

    lax.fori_loop(0, SR, to_rows, 0)

    def take_in(image, plane, line_place, there):
        x_ref[plane, line_place] = image_ref[image, there]

    each_image(size_ref, pair, take_in)

    def arrange(k, carry):
        total, square = carry
        rows = step_rows(k)
        for plane in range(4):
            share = shape.share(plane, k)
            inv_ref[plane, rows] = share
            values = jnp.where(share > 0.0, x_ref[plane, rows], 0.0)
            x_ref[plane, rows] = values
            total = total + fold(values)
            square = square + fold(values * values)
        return (total, square)

    nothing = jnp.zeros((8, C2), f32)
    total, square = sweep(arrange, (nothing, nothing))
    mean1, scaling1 = norm_terms(total, square, shape.count_two)
    factor1 = scaling1 * gain1
    shift1 = bias1 - mean1 * scaling1 * gain1

    def window_cols(k, carry):
        rows = step_rows(k)
        for pr in range(2):
            masked = []
            for pc in range(2):
                plane = pr * 2 + pc
                normal = rounded(affine(x_ref[plane, rows], factor1, shift1))
                masked.append(jnp.where(inv_ref[plane, rows] > 0.0, normal, 0.0))
            put_col_windows(col_ref, pr, k, *masked)
        return carry

    sweep(window_cols, 0)

    def mix(k, carry):
        total, square = carry
        rows = step_rows(k)
        for pc in range(2):
            windows = row_windows(col_ref, pc, k)
            for pr in range(2):
                plane = pr * 2 + pc
                values = x_ref[plane, rows]
                share = inv_ref[plane, rows]
                pooled = windows[pr] * share - rounded(affine(values, factor1, shift1))
                pooled = jnp.where(share > 0.0, pooled, 0.0)
                mixed = values + scale1 * pooled
                pool_ref[plane, rows] = pooled
                mix_ref[plane, rows] = mixed
                total = total + fold(mixed)
                square = square + fold(mixed * mixed)
        return (total, square)

    total, square = sweep(mix, (nothing, nothing))
    mean2, scaling2 = norm_terms(total, square, shape.count_two)
    for n, value in enumerate((mean1, scaling1, mean2, scaling2)):
        stat_out[0, n] = spread(value, 128)


def pair_specs(pairs, shapes, mode=None):
    if pairs == 1:
        return [VMEM_BLOCK] * len(shapes)
    return [
        pl.BlockSpec(
            (1,) + shape, lambda t, rank=len(shape): (t,) + (0,) * rank, pipeline_mode=mode
        )
        for shape in shapes
    ]


def whole_specs(pairs, shapes):
    if pairs == 1:
        return [VMEM_BLOCK] * len(shapes)
    return [
        pl.BlockSpec(
            shape,
            lambda t, rank=len(shape): (0,) * rank,
            pipeline_mode=pl.Buffered(1),
        )
        for shape in shapes
    ]


def pair_arrays(pairs, shapes, kinds):
    make = pltpu.VMEM if pairs == 1 else jax.ShapeDtypeStruct
    return [make((pairs,) + shape, kind) for shape, kind in zip(shapes, kinds)]


STATE = [(4, AREA, C2)] * 4 + [(4, 8, 128)]
BACK = [(4, AREA, C2)] * 2 + [(2, 8, 128)]


def run_entry(sizes, strips, vec_two):
    strip_count = strips.shape[0]
    pairs = strip_count // 8
    return pl.pallas_call(
        functools.partial(entry_kernel, pairs, strip_count),
        grid=() if pairs == 1 else (pairs,),
        in_specs=[SMEM] + whole_specs(pairs, [strips.shape, vec_two.shape]),
        out_specs=pair_specs(pairs, STATE),
        out_shape=pair_arrays(pairs, STATE, [f32] * 5),
        scratch_shapes=[
            pltpu.VMEM((2, CH * LINE, C2), f32),
            pltpu.VMEM((4, AREA + 2 * LINE, C2), f32),
        ],
        compiler_params=roomy(6 if pairs == 1 else 40),
        name="entry",
    )(sizes, strips, vec_two)


WEIGHTS = [(C2, HID2), (HID2, C2), (9 * C2, WIDE), (WIDE, HID3), (HID3, WIDE)]


def unpack_kernel(piece_count, slot_ref, *refs):
    piece_refs, refs = refs[:piece_count], refs[piece_count:]
    weights, gathered_ref = refs[:-1], refs[-1]
    count = piece_refs[0].shape[0]
    for n, ref in enumerate(piece_refs):
        gathered_ref[n * count : n * count + count] = ref[...]
    left_half = lax.broadcasted_iota(jnp.int32, (HALF, 128), 1) < BS
    offset = 0
    for (rows, cols), ref in zip(SHAPES, weights):
        wide = cols // BS
        for rb in range(rows // BS):
            for cb in range(0, wide, 2):
                number = offset + rb * wide + cb
                first = gathered_ref[slot_ref[number]]
                turned = pltpu.roll(first, BS, 1)
                if cb + 1 < wide:
                    second = gathered_ref[slot_ref[number + 1]]
                    top = jnp.where(left_half, first, pltpu.roll(second, BS, 1))
                    low = jnp.where(left_half, turned, second)
                else:
                    top = jnp.where(left_half, first, 0.0)
                    low = jnp.where(left_half, turned, 0.0)
                place = slice(cb * BS, cb * BS + 128)
                ref[rb * BS : rb * BS + HALF, place] = top
                ref[rb * BS + HALF : rb * BS + BS, place] = low
        offset += rows // BS * wide
    weights[3][C3:, :] = jnp.zeros((WIDE - C3, HID3), bf16)


def run_unpack(slot_of, pieces):
    slots = sum(piece.shape[0] for piece in pieces)
    return pl.pallas_call(
        functools.partial(unpack_kernel, len(pieces)),
        in_specs=[SMEM] + [VMEM_BLOCK] * len(pieces),
        out_specs=[VMEM_BLOCK] * 5,
        out_shape=[pltpu.VMEM(shape, bf16) for shape in WEIGHTS],
        scratch_shapes=[pltpu.VMEM((slots, HALF, 128), bf16)],
        compiler_params=roomy(6),
        name="unpack",
    )(slot_of, *held_in(pltpu.VMEM, *pieces))


def main_kernel(
    pairs,
    strip_count,
    slots,
    near_place,
    far_place,
    size_ref,
    inv_in,
    mix_in,
    stat_in,
    goal_ref,
    vec_two_ref,
    vec_hid_two_ref,
    vec_three_ref,
    vec_hid_three_ref,
    w1_ref,
    w2_ref,
    we_ref,
    w3_ref,
    w4_ref,
    result_ref,
    zed_out,
    dx_out,
    mean_out,
    near_ref,
    far_ref,
    flat_ref,
    zed_ref,
    hid_ref,
    u_ref,
    g_ref,
    h_ref,
    dy_ref,
    patch_ref,
    dpatch_ref,
    inv3_ref,
    e_ref,
    col3_ref,
    pool3_ref,
    mix3_ref,
    dx3_ref,
    hid3_ref,
    dhid3_ref,
    u3_ref,
    g3_ref,
    h3_ref,
    dy3_ref,
    dpre_ref,
    gw1_ref,
    gw2_ref,
    gwe_ref,
    gw3_ref,
    gw4_ref,
    acc_two,
    acc_hid_two,
    acc_three,
    acc_hid_three,
):
    pair = pl.program_id(0) if pairs > 1 else 0
    grads = [gw1_ref, gw2_ref, gwe_ref, gw3_ref, gw4_ref]
    inv_ref, mix_ref, stat_ref = (ref.at[0] for ref in (inv_in, mix_in, stat_in))
    back_ref, dx_ref = zed_out.at[0], dx_out.at[0]
    left_half = lax.broadcasted_iota(jnp.int32, (HALF, 128), 1) < BS

    def at_pair(number, act):
        if pairs == 1:
            act()
        else:
            pl.when(pair == number)(act)

    def begin():
        acc_two[...] = jnp.zeros(acc_two.shape, f32)
        acc_hid_two[...] = jnp.zeros(acc_hid_two.shape, f32)
        acc_three[...] = jnp.zeros(acc_three.shape, f32)
        acc_hid_three[...] = jnp.zeros(acc_hid_three.shape, f32)

    at_pair(0, begin)
    shape = Geometry(size_ref, pair)
    count_two, count_three, flipped = shape.count_two, shape.count_three, shape.flipped
    nothing = jnp.zeros((8, C2), f32)
    nothing3 = jnp.zeros((8, WIDE), f32)
    gain2, bias2, scale2, out_bias = (vec_two_ref[n : n + 1] for n in range(3, 7))
    embed_bias, gain3, bias3, scale3 = (vec_three_ref[n : n + 1] for n in range(4))
    gain4, bias4, scale4, out_bias3 = (vec_three_ref[n : n + 1] for n in range(4, 8))
    mean2, scaling2 = stat_ref[2], stat_ref[3]
    factor2 = scaling2 * gain2
    shift2 = bias2 - mean2 * scaling2 * gain2
    for plane in range(4):
        zed_ref[plane, 0:LINE] = jnp.zeros((LINE, C2), f32)
    col3_ref[0:LINE] = jnp.zeros((LINE, WIDE), f32)
    col3_ref[AREA + LINE : AREA + 2 * LINE] = jnp.zeros((LINE, WIDE), f32)

    def put_block(number, block):
        near_ref[near_place[number]] = block
        far_ref[far_place[number]] = block

    def pack_blocks(matrices):
        offsets = [0]
        for rows, cols in SHAPES:
            offsets.append(offsets[-1] + rows // BS * (cols // BS))
        for which in matrices:
            (rows, cols), ref = SHAPES[which], grads[which]
            wide = cols // BS
            for rb in range(rows // BS):
                for cb in range(0, wide, 2):
                    number = offsets[which] + rb * wide + cb
                    at = slice(cb * BS, cb * BS + 128)
                    top = ref[rb * BS : rb * BS + HALF, at].astype(bf16)
                    low = ref[rb * BS + HALF : rb * BS + BS, at].astype(bf16)
                    put_block(number, jnp.where(left_half, top, pltpu.roll(low, BS, 1)))
                    if cb + 1 < wide:
                        put_block(number + 1, jnp.where(left_half, pltpu.roll(top, BS, 1), low))

    def plane_rows(plane):
        return slice(plane * AREA, plane * AREA + AREA)

    def begin_plane(plane):
        low = affine(mix_ref[plane], factor2, shift2).astype(bf16)
        h_ref[plane_rows(plane)] = low
        hid_ref[plane % 2] = product(low, w1_ref[...])

    begin_plane(0)
    for plane in range(4):
        if plane < 3:
            begin_plane(plane + 1)
        for k in range(STEPS):
            rows = step_rows(k)
            flat = slice(plane * AREA + k * STEP, plane * AREA + k * STEP + STEP)
            for at in range(0, HID2, 128):
                lanes = slice(at, at + 128)
                active, slope = gelu_pair(hid_ref[plane % 2, rows, lanes] + vec_hid_two_ref[:, lanes])
                u_ref[flat, lanes] = active.astype(bf16)
                g_ref[flat, lanes] = slope.astype(bf16)
        out = product(u_ref[plane_rows(plane)], w2_ref[...]) + out_bias
        zed = jnp.where(inv_ref[plane] > 0.0, mix_ref[plane] + scale2 * out, 0.0)
        zed_ref[plane, LINE : LINE + AREA] = rounded(zed)

    def patches(k, carry):
        rows = step_rows(k)
        taps = []
        for ky in range(3):
            pr = (0 if ky == 1 else 1) * 2
            source = step_rows(k, 0 if ky == 0 else 1)
            even = zed_ref[pr, source]
            odd = zed_ref[pr + 1, source]
            taps.append((from_left(odd), even, odd))
        for ky in range(3):
            for kx in range(3):
                at = (3 * ky + kx) * C2
                tap = taps[ky][kx]
                if ky != kx:
                    tap = jnp.where(flipped, taps[kx][ky], tap)
                patch_ref[rows, at : at + C2] = tap.astype(bf16)
        return carry

    sweep(patches, 0)
    e_ref[...] = product(patch_ref[...], we_ref[...])

    def embed(k, carry):
        total, square = carry
        rows = step_rows(k)
        share = shape.share3(k)
        inv3_ref[rows] = share
        out = jnp.where(widen(share) > 0.0, e_ref[rows] + embed_bias, 0.0)
        e_ref[rows] = out
        return (total + fold(out), square + fold(out * out))

    total, square = sweep(embed, (nothing3, nothing3))
    mean3, scaling3 = norm_terms(total, square, count_three)
    factor3 = scaling3 * gain3
    shift3 = bias3 - mean3 * scaling3 * gain3

    def window_cols3(k, carry):
        rows = step_rows(k)
        normal = rounded(affine(e_ref[rows], factor3, shift3))
        masked = jnp.where(widen(inv3_ref[rows]) > 0.0, normal, 0.0)
        col3_ref[step_rows(k, 1)] = masked + from_left(masked) + from_right(masked)
        return carry

    sweep(window_cols3, 0)

    def row_windows3(k):
        return col3_ref[step_rows(k)] + col3_ref[step_rows(k, 1)] + col3_ref[step_rows(k, 2)]

    def mix3(k, carry):
        total, square = carry
        rows = step_rows(k)
        values = e_ref[rows]
        share = widen(inv3_ref[rows])
        pooled = row_windows3(k) * share - rounded(affine(values, factor3, shift3))
        pooled = jnp.where(share > 0.0, pooled, 0.0)
        mixed = values + scale3 * pooled
        pool3_ref[rows] = pooled
        mix3_ref[rows] = mixed
        return (total + fold(mixed), square + fold(mixed * mixed))

    total, square = sweep(mix3, (nothing3, nothing3))
    mean4, scaling4 = norm_terms(total, square, count_three)
    factor4 = scaling4 * gain4
    shift4 = bias4 - mean4 * scaling4 * gain4
    normal4 = (spread(scaling4, WIDE), spread(-mean4 * scaling4, WIDE))

    def prepare3(k, d_bias):
        rows = step_rows(k)
        h3_ref[rows] = affine(mix3_ref[rows], factor4, shift4).astype(bf16)
        goal = goal_ref[0, rows].astype(f32)
        goal = jnp.where(widen(inv3_ref[rows]) > 0.0, goal, 0.0)
        low_goal = (scale4 * goal).astype(bf16)
        dy3_ref[rows] = low_goal
        return d_bias + fold(low_goal.astype(f32))

    acc_three[7] += sweep(prepare3, nothing3)

    def keep(ref, value, place=slice(None)):
        if pairs == 1:
            ref[place] = value.astype(ref.dtype)
        else:

            @pl.when(pair == 0)
            def _():
                ref[place] = value

            @pl.when(pair > 0)
            def _():
                ref[place] += value

    def begin_chunk(at):
        lanes = slice(at, at + 256)
        hid3_ref[:, lanes] = product(h3_ref[...], w3_ref[:, lanes])
        dhid3_ref[:, lanes] = product_nt(dy3_ref[...], w4_ref[lanes])

    begin_chunk(0)
    for at in range(0, HID3, 256):
        if at + 256 < HID3:
            begin_chunk(at + 256)
        for lane in (at, at + 128):
            lanes = slice(lane, lane + 128)
            total = nothing
            for k in range(STEPS):
                rows = step_rows(k)
                active, slope = gelu_pair(hid3_ref[rows, lanes] + vec_hid_three_ref[:, lanes])
                u3_ref[rows, lanes] = active.astype(bf16)
                low = (slope * dhid3_ref[rows, lanes]).astype(bf16)
                g3_ref[rows, lanes] = low
                total = total + fold(low.astype(f32))
            acc_hid_three[:, lanes] += total
        lanes = slice(at, at + 256)
        out = product(u3_ref[:, lanes], w4_ref[lanes])
        d_low = product_nt(g3_ref[:, lanes], w3_ref[:, lanes])
        result_ref[0] = out if at == 0 else result_ref[0] + out
        dx3_ref[...] = d_low if at == 0 else dx3_ref[...] + d_low
        keep(gw3_ref, product_tn(h3_ref[...], g3_ref[:, lanes]), (slice(None), lanes))
        keep(gw4_ref, product_tn(u3_ref[:, lanes], dy3_ref[...]), lanes)

    def finish3(k, carry):
        d_scale, d_shift, d_gain = carry
        rows = step_rows(k)
        valid = widen(inv3_ref[rows]) > 0.0
        mixed = mix3_ref[rows]
        out = jnp.where(valid, result_ref[0, rows] + out_bias3, 0.0)
        result_ref[0, rows] = mixed + scale4 * out
        d_scale = d_scale + fold(out * goal_ref[0, rows].astype(f32))
        d_low = dx3_ref[rows]
        normal = affine(mixed, *normal4)
        return (d_scale, d_shift + fold(d_low), d_gain + fold(d_low * normal))

    d_scale, d_shift, d_gain = sweep(finish3, (nothing3, nothing3, nothing3))
    acc_three[6] += d_scale
    acc_three[5] += d_shift
    acc_three[4] += d_gain
    mean_shift = by_image(d_shift * gain4) / count_three
    mean_gain = by_image(d_gain * gain4) / count_three
    back_gain4 = scaling4 * gain4
    back_mean4 = spread(-scaling4 * mean_shift, WIDE)
    back_normal4 = spread(scaling4 * mean_gain, WIDE)

    def unmix3(k, d_scale):
        rows = step_rows(k)
        share = widen(inv3_ref[rows])
        valid = share > 0.0
        normal = affine(mix3_ref[rows], *normal4)
        back = affine(dx3_ref[rows], back_gain4, back_mean4) - scaled(normal, back_normal4)
        d_mixed = jnp.where(valid, back + goal_ref[0, rows].astype(f32), 0.0)
        dx3_ref[rows] = d_mixed
        d_scale = d_scale + fold(pool3_ref[rows] * d_mixed)
        weighted = scale3 * d_mixed * share
        col3_ref[step_rows(k, 1)] = weighted + from_left(weighted) + from_right(weighted)
        return d_scale

    acc_three[3] += sweep(unmix3, nothing3)
    normal3 = (spread(scaling3, WIDE), spread(-mean3 * scaling3, WIDE))

    def unpool3(k, carry):
        d_shift, d_gain = carry
        rows = step_rows(k)
        valid = widen(inv3_ref[rows]) > 0.0
        d_normal = jnp.where(valid, row_windows3(k) - scale3 * dx3_ref[rows], 0.0)
        pool3_ref[rows] = d_normal
        normal = affine(e_ref[rows], *normal3)
        return (d_shift + fold(d_normal), d_gain + fold(d_normal * normal))

    d_shift, d_gain = sweep(unpool3, (nothing3, nothing3))
    acc_three[2] += d_shift
    acc_three[1] += d_gain
    mean_shift = by_image(d_shift * gain3) / count_three
    mean_gain = by_image(d_gain * gain3) / count_three
    back_gain3 = scaling3 * gain3
    back_mean3 = spread(-scaling3 * mean_shift, WIDE)
    back_normal3 = spread(scaling3 * mean_gain, WIDE)

    def unnorm3(k, d_bias):
        rows = step_rows(k)
        valid = widen(inv3_ref[rows]) > 0.0
        normal = affine(e_ref[rows], *normal3)
        back = affine(pool3_ref[rows], back_gain3, back_mean3) - scaled(normal, back_normal3)
        low = jnp.where(valid, dx3_ref[rows] + back, 0.0).astype(bf16)
        dpre_ref[rows] = low
        return d_bias + fold(low.astype(f32))

    acc_three[0] += sweep(unnorm3, nothing3)
    keep(gwe_ref, product_tn(patch_ref[...], dpre_ref[...]))
    dpatch_ref[0:AREA] = product_nt(dpre_ref[...], we_ref[...])
    dpatch_ref[AREA : AREA + LINE] = jnp.zeros((LINE, 9 * C2), f32)

    def gather_back(k, carry):
        rows = step_rows(k)

        def tap(ky, kx, source):
            at = (3 * ky + kx) * C2
            value = dpatch_ref[source, at : at + C2]
            if ky != kx:
                at = (3 * kx + ky) * C2
                value = jnp.where(flipped, dpatch_ref[source, at : at + C2], value)
            return value

        sources = []
        for ky in range(3):
            source = step_rows(k, 1 if ky == 0 else 0)
            sources.append(
                (tap(ky, 1, source), tap(ky, 2, source) + from_right(tap(ky, 0, source)))
            )
        for pc in range(2):
            for pr, value in ((0, sources[1][pc]), (1, sources[2][pc] + sources[0][pc])):
                plane = pr * 2 + pc
                valid = inv_ref[plane, rows] > 0.0
                back_ref[plane, rows] = jnp.where(valid, rounded(value), 0.0)
        return carry

    sweep(gather_back, 0)

    if pairs == 1:
        pack_blocks(range(2, 5))

    normal2 = (spread(scaling2, C2), spread(-mean2 * scaling2, C2))

    def begin_back(plane):
        low_goal = (scale2 * back_ref[plane]).astype(bf16)
        dy_ref[plane_rows(plane)] = low_goal
        hid_ref[plane % 2] = product_nt(low_goal, w2_ref[...])
        return fold(low_goal.astype(f32))

    d_out_bias = begin_back(0)
    d_shift, d_gain = nothing, nothing
    sums = [nothing] * (HID2 // 128)
    new_gw1, new_gw2 = None, None
    for plane in range(4):
        if plane < 3:
            d_out_bias = d_out_bias + begin_back(plane + 1)
        for k in range(STEPS):
            rows = step_rows(k)
            part = slice(plane * AREA + k * STEP, plane * AREA + k * STEP + STEP)
            for n, at in enumerate(range(0, HID2, 128)):
                lanes = slice(at, at + 128)
                low = g_ref[part, lanes].astype(f32) * hid_ref[plane % 2, rows, lanes]
                low = low.astype(bf16)
                g_ref[part, lanes] = low
                sums[n] = sums[n] + fold(low.astype(f32))
        flat = plane_rows(plane)
        d_low = product_nt(g_ref[flat], w1_ref[...])
        dx_ref[plane] = d_low
        d_shift = d_shift + fold(d_low)
        d_gain = d_gain + fold(d_low * affine(mix_ref[plane], *normal2))
        part_gw1 = product_tn(h_ref[flat], g_ref[flat])
        part_gw2 = product_tn(dy_ref[flat], u_ref[flat])
        new_gw1 = part_gw1 if plane == 0 else new_gw1 + part_gw1
        new_gw2 = part_gw2 if plane == 0 else new_gw2 + part_gw2
    new_gw2 = new_gw2.T
    for n, value in enumerate(sums):
        acc_hid_two[:, n * 128 : n * 128 + 128] += value
    acc_two[6] += d_out_bias
    acc_two[4] += d_shift
    acc_two[3] += d_gain
    mean_out[0, 0] = spread(by_image(d_shift * gain2) / count_two, 128)
    mean_out[0, 1] = spread(by_image(d_gain * gain2) / count_two, 128)
    keep(gw1_ref, new_gw1)
    keep(gw2_ref, new_gw2)
    d_scale = fold(w2_ref[...].astype(f32) * new_gw2) + out_bias * d_out_bias
    acc_two[5] += d_scale / scale2

    def finish():
        if pairs > 1:
            pack_blocks(range(5))
        else:
            pack_blocks(range(2))

        def filler(number, carry):
            put_block(number, jnp.zeros((HALF, 128), bf16))
            return carry

        lax.fori_loop(USED, slots, filler, 0)

        flat_ref[...] = jnp.zeros(flat_ref.shape, f32)

        def put(at, total, length):
            if at % 128:
                room = jnp.zeros((8, 128), f32)
                if total.shape[1] < length + BS:
                    total = jnp.concatenate([total, room], axis=1)
                total = pltpu.roll(total, BS, 1)
            whole = jnp.sum(total, axis=0, keepdims=True)
            done = -(at % 128)
            row = at // 128
            lane = 0
            while done < length:
                first = max(0, -done)
                last = min(128, length - done)
                flat_ref[row : row + 1, first:last] = whole[:, lane + first : lane + last]
                done += 128
                lane += 128
                row += 1

        at = 3 * C2
        for n in range(3, 6):
            put(at, acc_two[n], C2)
            at += C2
        put(at, acc_hid_two[...], HID2)
        at += HID2
        put(at, acc_two[6], C2)
        at += C2
        for n in range(7):
            put(at, acc_three[n], C3)
            at += C3
        put(at, acc_hid_three[...], HID3)
        at += HID3
        put(at, acc_three[7], C3)

    at_pair(pairs - 1, finish)


def run_main(places, sizes, state, goal, vectors, weights, strip_count):
    pairs = goal.shape[0]
    slots = places[0].shape[0]
    half = slots // 2 + 1
    if pairs == 1:
        state = held_in(pltpu.VMEM, *state)
    weights = held_in(pltpu.VMEM, *weights)
    _, inv, _, mix, stat = state
    state_shapes = [STATE[1], STATE[3], STATE[4]]
    grad_kind = bf16 if pairs == 1 else f32
    wide_f32 = pltpu.VMEM((AREA, WIDE), f32)
    wide_bf16 = pltpu.VMEM((AREA, WIDE), bf16)
    scratch = [
        pltpu.VMEM((4, AREA + LINE, C2), f32),
        pltpu.VMEM((2, AREA, HID2), f32),
        pltpu.VMEM((4 * AREA, HID2), bf16),
        pltpu.VMEM((4 * AREA, HID2), bf16),
        pltpu.VMEM((4 * AREA, C2), bf16),
        pltpu.VMEM((4 * AREA, C2), bf16),
        pltpu.VMEM((AREA, 9 * C2), bf16),
        pltpu.VMEM((AREA + LINE, 9 * C2), f32),
        pltpu.VMEM((AREA, 128), f32),
        wide_f32,
        pltpu.VMEM((AREA + 2 * LINE, WIDE), f32),
        wide_f32,
        wide_f32,
        wide_f32,
        pltpu.VMEM((AREA, HID3), f32),
        pltpu.VMEM((AREA, HID3), f32),
        pltpu.VMEM((AREA, HID3), bf16),
        pltpu.VMEM((AREA, HID3), bf16),
        wide_bf16,
        wide_bf16,
        wide_bf16,
        pltpu.VMEM((C2, HID2), grad_kind),
        pltpu.VMEM((HID2, C2), grad_kind),
        pltpu.VMEM((9 * C2, WIDE), grad_kind),
        pltpu.VMEM((WIDE, HID3), grad_kind),
        pltpu.VMEM((HID3, WIDE), grad_kind),
        pltpu.VMEM((7, 8, C2), f32),
        pltpu.VMEM((8, HID2), f32),
        pltpu.VMEM((8, 8, WIDE), f32),
        pltpu.VMEM((8, HID3), f32),
    ]
    out_shapes = [(half, HALF, 128), (half, HALF, 128), (VEC_BLOCKS * HALF, 128)]
    make = pltpu.VMEM if pairs == 1 else jax.ShapeDtypeStruct
    return pl.pallas_call(
        functools.partial(main_kernel, pairs, strip_count, slots),
        grid=() if pairs == 1 else (pairs,),
        in_specs=[SMEM] * 3
        + pair_specs(pairs, state_shapes + [goal.shape[1:]], pl.Buffered(1))
        + whole_specs(pairs, [vector.shape for vector in vectors])
        + [VMEM_BLOCK] * 5,
        out_specs=pair_specs(pairs, [(AREA, WIDE)] + BACK) + whole_specs(pairs, out_shapes),
        out_shape=pair_arrays(pairs, [(AREA, WIDE)] + BACK, [f32] * 4)
        + [make(shape, kind) for shape, kind in zip(out_shapes, (bf16, bf16, f32))],
        scratch_shapes=scratch,
        compiler_params=pltpu.CompilerParams(
            vmem_limit_bytes=(40 if pairs == 1 else 56) * 1024 * 1024,
            fuse_transposed_lhs_in_matmul=True,
        ),
        name="blocks",
    )(*places, sizes, inv, mix, stat, goal, *vectors, *weights)


def exit_kernel(
    pairs,
    strip_count,
    size_ref,
    x_in,
    inv_in,
    pool_in,
    mix_in,
    stat_in,
    zed_in,
    dx_in,
    mean_in,
    flat_ref,
    vec_two_ref,
    payload_hbm,
    vector_ref,
    payload_ref,
    image_ref,
    col_ref,
    dx_ref,
    back_ref,
    acc_ref,
    sem,
):
    pair = pl.program_id(0) if pairs > 1 else 0
    x_ref, inv_ref, pool_ref, mix_ref, stat_ref, zed_ref, low_ref, mean_ref = (
        ref.at[0] for ref in (x_in, inv_in, pool_in, mix_in, stat_in, zed_in, dx_in, mean_in)
    )
    shape = Geometry(size_ref, pair)
    count_two = shape.count_two
    gain1, bias1, scale1, gain2 = (vec_two_ref[n : n + 1] for n in range(4))
    mean1, scaling1, mean2, scaling2 = (stat_ref[n] for n in range(4))
    normal2 = (scaling2, -mean2 * scaling2)
    clear_edges(col_ref)
    nothing = jnp.zeros((8, C2), f32)
    back_gain2 = scaling2 * gain2
    back_mean2 = -scaling2 * mean_ref[0]
    back_normal2 = scaling2 * mean_ref[1]

    if pairs > 1:

        @pl.when(pair == 0)
        def _():
            acc_ref[...] = jnp.zeros(acc_ref.shape, f32)

    def add_up(n, total):
        acc_ref[n] = total if pairs == 1 else acc_ref[n] + total

    def unmix(k, d_scale):
        rows = step_rows(k)
        for pr in range(2):
            weighted = []
            for pc in range(2):
                plane = pr * 2 + pc
                share = inv_ref[plane, rows]
                normal = affine(mix_ref[plane, rows], *normal2)
                back = affine(low_ref[plane, rows], back_gain2, back_mean2)
                back = back - scaled(normal, back_normal2)
                d_mixed = jnp.where(share > 0.0, zed_ref[plane, rows] + back, 0.0)
                dx_ref[plane, rows] = d_mixed
                d_scale = d_scale + fold(pool_ref[plane, rows] * d_mixed)
                weighted.append(scale1 * d_mixed * share)
            put_col_windows(col_ref, pr, k, *weighted)
        return d_scale

    add_up(2, sweep(unmix, nothing))
    normal1 = (spread(scaling1, C2), spread(-mean1 * scaling1, C2))

    def unpool(k, carry):
        d_shift, d_gain = carry
        rows = step_rows(k)
        for pc in range(2):
            windows = row_windows(col_ref, pc, k)
            for pr in range(2):
                plane = pr * 2 + pc
                valid = inv_ref[plane, rows] > 0.0
                d_normal = windows[pr] - scale1 * dx_ref[plane, rows]
                d_normal = jnp.where(valid, d_normal, 0.0)
                back_ref[plane, rows] = d_normal
                normal = affine(x_ref[plane, rows], *normal1)
                d_shift = d_shift + fold(d_normal)
                d_gain = d_gain + fold(d_normal * normal)
        return (d_shift, d_gain)

    d_shift, d_gain = sweep(unpool, (nothing, nothing))
    add_up(1, d_shift)
    add_up(0, d_gain)
    mean_shift = by_image(d_shift * gain1) / count_two
    mean_gain = by_image(d_gain * gain1) / count_two
    back_gain1 = scaling1 * gain1
    back_mean1 = spread(-scaling1 * mean_shift, C2)
    back_normal1 = spread(scaling1 * mean_gain, C2)

    def unnorm(k, carry):
        rows = step_rows(k)
        for plane in range(4):
            normal = affine(x_ref[plane, rows], *normal1)
            back = affine(back_ref[plane, rows], back_gain1, back_mean1)
            back = back - scaled(normal, back_normal1)
            valid = inv_ref[plane, rows] > 0.0
            dx_ref[plane, rows] = jnp.where(valid, dx_ref[plane, rows] + back, 0.0)
        return carry

    sweep(unnorm, 0)

    def give_back(image, plane, line_place, there):
        image_ref[image, there] = dx_ref[plane, line_place]

    image_ref[...] = jnp.zeros(image_ref.shape, f32)
    each_image(size_ref, pair, give_back)

    def from_rows(within, carry):
        for spot in range(2 * STRIPS):
            image, strip = spot // STRIPS, spot % STRIPS
            start = pl.multiple_of((strip * SR + within) * LINE, LINE)
            target = strip_place(pair, spot, strip_count)
            payload_ref[target, within] = image_ref[image, pl.ds(start, CW)].astype(bf16)
        return carry

    lax.fori_loop(0, SR, from_rows, 0)

    def finish():
        copy = pltpu.make_async_copy(payload_ref, payload_hbm, sem)
        copy.start()
        vector_ref[...] = flat_ref[...]
        for n in range(3):
            vector_ref[n : n + 1] = jnp.sum(acc_ref[n], axis=0, keepdims=True)
        copy.wait()

    if pairs == 1:
        finish()
    else:
        pl.when(pair == pairs - 1)(finish)


def run_exit(sizes, state, back, flat, vec_two, strip_count):
    pairs = strip_count // 8
    payload = (strip_count, SR, CW, C2)
    make = pltpu.VMEM if pairs == 1 else jax.ShapeDtypeStruct
    plane_f32 = pltpu.VMEM((4, AREA, C2), f32)
    arrays = [*state, *back]
    if pairs == 1:
        arrays = held_in(pltpu.VMEM, *arrays)
    return pl.pallas_call(
        functools.partial(exit_kernel, pairs, strip_count),
        grid=() if pairs == 1 else (pairs,),
        in_specs=[SMEM]
        + pair_specs(pairs, STATE + BACK, pl.Buffered(1))
        + whole_specs(pairs, [flat.shape, vec_two.shape]),
        out_specs=[HBM] + whole_specs(pairs, [flat.shape]),
        out_shape=[pltpu.HBM(payload, bf16), make(flat.shape, f32)],
        scratch_shapes=[
            pltpu.VMEM(payload, bf16),
            pltpu.VMEM((2, CH * LINE, C2), f32),
            pltpu.VMEM((4, AREA + 2 * LINE, C2), f32),
            plane_f32,
            plane_f32,
            pltpu.VMEM((3, 8, C2), f32),
            pltpu.SemaphoreType.DMA,
        ],
        compiler_params=roomy(8 if pairs == 1 else 40),
        name="exit",
    )(sizes, *arrays, flat, vec_two)


def pack_kernel(master_ref, dense_ref):
    values = master_ref[...]
    dense_ref[...] = jnp.concatenate([values[:, :HALF], values[:, HALF:]], axis=2).astype(bf16)


def pack(master):
    owned = master.shape[0]
    return pl.pallas_call(
        pack_kernel,
        out_shape=jax.ShapeDtypeStruct((owned, HALF, 2 * BS), bf16),
        name="pack",
    )(master)


def fold_pair_kernel(near_ref, got_ref, own_ref, *part_refs):
    share = own_ref.shape[0]

    def one(n, carry):
        for k in range(len(part_refs) + 1):
            total = near_ref[k * share + n].astype(f32) + got_ref[k * share + n].astype(f32)
            if k == 0:
                own_ref[n] = total
            else:
                part_refs[k - 1][n] = total.astype(bf16)
        return carry

    lax.fori_loop(0, share, one, 0, unroll=4)


def fold_pair(near, got, groups):
    shape = ((near.shape[0] - 1) // groups,) + near.shape[1:]
    return pl.pallas_call(
        fold_pair_kernel,
        in_specs=[VMEM_BLOCK] * 2,
        out_specs=[VMEM_BLOCK] * groups,
        out_shape=[pltpu.VMEM(shape, f32)] + [pltpu.VMEM(shape, bf16)] * (groups - 1),
        compiler_params=roomy(4),
        name="fold_pair",
    )(*held_in(pltpu.VMEM, near, got))


def fold_tile_kernel(pieces, spot_ref, *refs):
    piece_refs, refs = refs[:pieces], refs[pieces:]
    vector_refs, refs = refs[:pieces], refs[pieces:]
    out_refs, sum_ref = refs[:-1], refs[-1]
    groups = len(out_refs)
    share = out_refs[0].shape[0]
    owned = piece_refs[0].shape[0]
    total = vector_refs[0][...]
    for ref in vector_refs[1:]:
        total = total + ref[...]
    for n in range(sum_ref.shape[0]):
        sum_ref[n] = jnp.zeros((HALF, 128), f32)
    for n in range(VEC_BLOCKS):
        sum_ref[n] = total[n * HALF : (n + 1) * HALF]

    def one(n, carry):
        for k, out_ref in enumerate(out_refs):
            number = lax.rem(spot_ref[0] + k, groups) * share + n
            block = jnp.minimum(number, owned - 1)
            total = piece_refs[0][block].astype(f32)
            for ref in piece_refs[1:]:
                total = total + ref[block].astype(f32)
            rest = sum_ref[jnp.maximum(number - owned, 0)]
            out_ref[n] = jnp.where(number < owned, total, rest).astype(out_ref.dtype)
        return carry

    lax.fori_loop(0, share, one, 0, unroll=share <= 16)


def fold_tile(spot, pieces, vectors, extra, groups):
    shape = ((pieces[0].shape[0] + extra) // groups,) + pieces[0].shape[1:]
    return pl.pallas_call(
        functools.partial(fold_tile_kernel, len(pieces)),
        in_specs=[SMEM] + [VMEM_BLOCK] * (len(pieces) + len(vectors)),
        out_specs=[VMEM_BLOCK] * groups,
        out_shape=[pltpu.VMEM(shape, f32)] + [pltpu.VMEM(shape, bf16)] * (groups - 1),
        scratch_shapes=[pltpu.VMEM((extra, HALF, 128), f32)],
        compiler_params=roomy(8),
        name="fold_tile",
    )(spot, *held_in(pltpu.VMEM, *pieces, *vectors))


def fold_batch_kernel(owned, vector_weight, spot_ref, *refs):
    part_refs, total_ref = refs[:-1], refs[-1]
    share = total_ref.shape[0] - 1
    square = jnp.zeros((8, 128), f32)
    for n in range(share):
        total = part_refs[0][n].astype(f32)
        for ref in part_refs[1:]:
            total = total + ref[n].astype(f32)
        total_ref[n] = total.astype(bf16)
        weight = jnp.where(spot_ref[0] * share + n < owned, 1.0, vector_weight)
        square = square + weight * fold(total * total)
    rest = 0.25 * jnp.sum(jnp.sum(square, axis=1, keepdims=True), axis=0, keepdims=True)
    row = lax.broadcasted_iota(jnp.int32, (HALF, 128), 0)
    block = jnp.zeros((HALF, 128), f32)
    for n in range(3):
        term = rounded(rest)
        block = jnp.where(row == n, term, block)
        rest = rest - term
    total_ref[share] = block.astype(bf16)


def fold_batch(spot, parts, owned, tile_count):
    shape = (parts[0].shape[0] + 1,) + parts[0].shape[1:]
    return pl.pallas_call(
        functools.partial(fold_batch_kernel, owned, 1.0 / tile_count),
        in_specs=[SMEM] + [VMEM_BLOCK] * len(parts),
        out_specs=VMEM_BLOCK,
        out_shape=pltpu.VMEM(shape, bf16),
        compiler_params=roomy(4),
        name="fold_batch",
    )(spot, *held_in(pltpu.VMEM, *parts))


def norm_kernel(spot_ref, *refs):
    quarters, sum_ref = refs[:-1], refs[-1]
    groups = len(quarters)
    share = quarters[0].shape[0] - 1
    total = jnp.zeros((1, 128), f32)
    for source in range(groups):
        turn = lax.rem(spot_ref[0] - source + groups, groups)
        terms = quarters[0][share].astype(f32)
        for k in range(1, groups):
            terms = jnp.where(turn == k, quarters[k][share].astype(f32), terms)
        total = total + 4.0 * (terms[0:1] + (terms[1:2] + terms[2:3]))
    sum_ref[...] = jnp.broadcast_to(total, sum_ref.shape)


def square_sum(spot, quarters):
    return pl.pallas_call(
        norm_kernel,
        in_specs=[SMEM] + [VMEM_BLOCK] * len(quarters),
        out_specs=VMEM_BLOCK,
        out_shape=pltpu.VMEM((8, 128), f32),
        compiler_params=roomy(4),
        name="norm",
    )(spot, *held_in(pltpu.VMEM, *quarters))


def update_kernel(owned, groups, spot_ref, *refs):
    norm_refs, quarters, refs = refs[:4], refs[4 : 4 + groups], refs[4 + groups :]
    stat_hbm, out_hbm, (vector_ref, clip_ref), refs = refs[:5], refs[5:10], refs[10:12], refs[12:]
    stat_refs, out_refs, (in_sem, out_sem) = refs[:5], refs[5:10], refs[10:]
    master_ref, left_stat_ref, right_stat_ref, left_root_ref, right_root_ref = stat_refs
    grad_ref, left_ref, right_ref, new_ref, copy_ref = out_refs
    share = quarters[0].shape[0] - 1
    spans = spans_of(owned)

    def copies_of(sources, targets, sems):
        return [
            [
                pltpu.make_async_copy(
                    source.at[pl.ds(*span)], target.at[pl.ds(*span)], sems.at[5 * n + k]
                )
                for k, (source, target) in enumerate(zip(sources, targets))
            ]
            for n, span in enumerate(spans)
        ]

    copies_in = copies_of(stat_hbm, stat_refs, in_sem)
    copies_out = copies_of(out_refs, out_hbm, out_sem)
    for copies in copies_in:
        for copy in copies:
            copy.start()
    total = [ref[0:1] for ref in norm_refs]
    norm = jnp.sqrt((total[0] + total[1]) + (total[2] + total[3]))
    factor = jnp.minimum(1.0, clip_limit / norm)
    left_half = lax.broadcasted_iota(jnp.int32, (HALF, 128), 1) < BS

    def summed(number):
        source = number // share
        local = number - source * share
        turn = lax.rem(spot_ref[0] - source + groups, groups)
        value = quarters[0][local].astype(f32)
        for k in range(1, groups):
            value = jnp.where(turn == k, quarters[k][local].astype(f32), value)
        return value * factor

    def side_by_side(first, count):
        sides = []
        for n in range(first, first + count, 2):
            dense = summed(n)
            turned = pltpu.roll(dense, BS, 1)
            if n + 1 < first + count:
                second = summed(n + 1)
                top = jnp.where(left_half, dense, pltpu.roll(second, BS, 1))
                low = jnp.where(left_half, turned, second)
                side = jnp.concatenate([top, low], axis=0)
                grad_ref[n + 1] = pltpu.roll(side, BS, 1)[:, :BS]
            else:
                side = jnp.concatenate([dense, turned], axis=0)[:, :BS]
            grad_ref[n] = side[:, :BS]
            sides.append(side.astype(bf16))
        return jnp.concatenate(sides, axis=1)

    def diagonal_of(count):
        order = (count * BS, count * BS)
        return lax.broadcasted_iota(jnp.int32, order, 0) // BS == (
            lax.broadcasted_iota(jnp.int32, order, 1) // BS
        )

    clip_ref[...] = norm
    for n in range(vector_ref.shape[0]):
        vector_ref[n] = summed(owned + n)
    for (first, length), arriving, leaving in zip(spans, copies_in, copies_out):
        parts = [(n, min(4, first + length - n)) for n in range(first, first + length, 4)]
        wides = [side_by_side(*part) for part in parts]
        tall = [
            jnp.where(diagonal_of(count), jnp.concatenate([wide] * count, axis=0), 0.0)
            for (_, count), wide in zip(parts, wides)
        ]
        lefts = [product_nt(one, wide) for one, wide in zip(tall, wides)]
        rights = [product_tn(wide, wide) for wide in wides]
        for copy in arriving:
            copy.wait()
        stepped = []
        for (start, count), wide in zip(parts, wides):
            roots = left_root_ref[pl.ds(start, count)].reshape(count * BS, BS).astype(bf16)
            stepped.append(product(roots, wide))
        for (start, count), left, right in zip(parts, lefts, rights):
            here = pl.ds(start, count)
            left_ref[here] = 0.5 * left_stat_ref[here] + 0.5 * left.reshape(count, BS, BS)
            for n in range(count):
                at = n // 2 * 128
                block = right[n * BS : n * BS + BS, at : min(at + 128, count * BS)]
                if n % 2:
                    block = pltpu.roll(block, BS, 1)
                right_ref[start + n] = 0.5 * right_stat_ref[start + n] + 0.5 * block[:, :BS]
        for (start, count), value in zip(parts, stepped):
            here = pl.ds(start, count)
            value = jnp.where(diagonal_of(count), value, 0.0).astype(bf16)
            roots = right_root_ref[here].reshape(count * BS, BS).astype(bf16)
            value = product(value, roots).reshape(count, BS, BS)
            new = master_ref[here] - rate_matrix * value
            new_ref[here] = new
            copy_ref[here] = new.astype(bf16)
        for copy in leaving:
            copy.start()
    for leaving in copies_out:
        for copy in leaving:
            copy.wait()


def spans_of(owned):
    spans = []
    first = 0
    while first < owned:
        length = min(8 if first == 0 else 12, owned - first)
        spans.append((first, length))
        first += length
    return spans


def update(spot, norms, quarters, extra, *stats):
    shape = stats[0].shape
    groups = len(quarters)
    types = [f32] * 4 + [bf16]
    steps = len(spans_of(shape[0]))
    return pl.pallas_call(
        functools.partial(update_kernel, shape[0], groups),
        in_specs=[SMEM] + [VMEM_BLOCK] * (groups + 4) + [HBM] * 5,
        out_specs=[HBM] * 5 + [VMEM_BLOCK] * 2,
        out_shape=[pltpu.HBM(shape, kind) for kind in types]
        + [
            jax.ShapeDtypeStruct((extra, HALF, 128), f32),
            jax.ShapeDtypeStruct((1, 128), f32),
        ],
        scratch_shapes=[pltpu.VMEM(shape, f32)] * 5
        + [pltpu.VMEM(shape, kind) for kind in types]
        + [
            pltpu.SemaphoreType.DMA((5 * steps,)),
            pltpu.SemaphoreType.DMA((5 * steps,)),
        ],
        compiler_params=roomy(20),
        name="update",
    )(spot, *held_in(pltpu.VMEM, *norms, *quarters), *held_in(pltpu.HBM, *stats))


def share_out(pieces, axis):
    return lax.all_to_all(pieces, axis, split_axis=0, concat_axis=0, tiled=True)


def swap(piece, distance):
    count = lax.axis_size("tile")
    return lax.ppermute(piece, "tile", [(i, i ^ distance) for i in range(count)])


def on_device(
    pixels,
    buckets,
    slot_owner_table,
    out_grad,
    master,
    left_stat,
    right_stat,
    left_root,
    right_root,
    vectors,
    moment,
):
    tile_count = lax.axis_size("tile")
    tile_place = lax.axis_index("tile")
    slot_count = pixels.shape[2]
    group_count = tile_count // STRIPS
    pairs = group_count // 2
    owned = master.shape[0]
    slots = owned * tile_count
    batch_count = lax.axis_size("batch")
    spot = lax.axis_index("batch").astype(jnp.int32).reshape(1)
    extra = extra_of(owned, batch_count)
    strips = share_out(pixels.reshape((tile_count,) + pixels.shape[3:]), "tile")
    dense = pack(master)
    paired = tile_count <= 8
    if paired:
        mine = [dense] + [swap(dense, 2 * k) for k in range(1, tile_count // 2)]
        pieces = mine + [swap(piece, 1) for piece in mine]
    else:
        pieces = [lax.all_gather(dense, "tile", axis=0, tiled=True)]

    numbers = jnp.arange(slots, dtype=jnp.int32)
    slot_of = jnp.sum(
        jnp.where(slot_owner_table[None, :] == numbers[:, None], numbers[None, :], 0), axis=1
    )
    owner = slot_of // owned
    within = slot_of - owner * owned
    place_of = slot_of
    if paired:
        apart = owner ^ tile_place
        apart = (apart & 1) * (tile_count // 2) + (apart >> 1)
        slot_of = place_of = within + owned * apart
    half = slots // 2
    near_place = jnp.where(place_of < half, place_of, half)
    far_place = jnp.where(place_of < half, half, place_of - half)
    image_ids = lax.dynamic_index_in_dim(
        buckets.reshape(group_count, slot_count), tile_place, 1, keepdims=False
    )
    turned = image_ids >= 2
    heights = jnp.where(image_ids == 0, 5 * CH // 9, jnp.where(image_ids == 1, 7 * CH // 9, CH))
    breadths = jnp.where(image_ids == 0, CW, jnp.where(image_ids == 1, 7 * CW // 9, 5 * CW // 9))
    sizes = jnp.stack(
        [
            jnp.where(turned, breadths, heights),
            jnp.where(turned, heights, breadths),
            turned,
        ],
        axis=1,
    )
    sizes = sizes.reshape(-1).astype(jnp.int32)

    two = 6 * C2 + HID2 + C2
    vec_two = jnp.concatenate([vectors[: 6 * C2], vectors[6 * C2 + HID2 : two]]).reshape(7, C2)
    vec_hid_two = vectors[6 * C2 : 6 * C2 + HID2].reshape(1, HID2)
    wide_end = two + 7 * C3
    vec_three = jnp.concatenate([vectors[two:wide_end], vectors[wide_end + HID3 :]])
    vec_three = jnp.pad(vec_three.reshape(8, C3), ((0, 0), (0, WIDE - C3)))
    vec_hid_three = vectors[wide_end : wide_end + HID3].reshape(1, HID3)

    flips = turned.reshape(-1, 1, 1, 1)
    goal = out_grad.reshape(2 * pairs, H3, W3, C3)
    goal = jnp.where(flips, goal.transpose(0, 2, 1, 3), goal)[:, :LINES]
    goal = goal.reshape(pairs, 2, LINES, W3, C3).transpose(0, 2, 3, 1, 4)
    goal = goal.reshape(pairs, LINES, 2 * W3, C3)
    goal = jnp.pad(goal, ((0, 0), (0, 0), (0, LINE - 2 * W3), (0, WIDE - C3)))
    goal = goal.reshape(pairs, AREA, WIDE)

    weights = run_unpack(slot_of, pieces)
    state = run_entry(sizes, strips, vec_two)
    result, *back, near, far, flat = run_main(
        (near_place, far_place),
        sizes,
        state,
        goal,
        (vec_two, vec_hid_two, vec_three, vec_hid_three),
        weights,
        tile_count,
    )
    pixel_back, vector = run_exit(sizes, state, back, flat, vec_two, tile_count)
    if paired:
        own, *parts = fold_pair(near, swap(far, 1), tile_count // 2)
        pieces = [own] + [swap(part, 2 * k + 2) for k, part in enumerate(parts)]
        vector, _ = lax.optimization_barrier((vector, parts[0]))
        vector = vector + swap(vector, 1)
        vectors_in = [vector] + [swap(vector, 2 * k) for k in range(1, tile_count // 2)]
    else:
        outgoing = jnp.concatenate([near[:half], far[:half]], axis=0)
        pieces = list(share_out(outgoing.reshape(tile_count, owned, HALF, 128), "tile"))
        vectors_in = list(lax.all_gather(vector, "tile"))
    result, pieces[1] = lax.optimization_barrier((result, pieces[1]))
    result = result.reshape(pairs, LINES, LINE, WIDE)[:, :, : 2 * W3, :C3]
    result = result.reshape(pairs, LINES, W3, 2, C3).transpose(0, 3, 1, 2, 4)
    result = result.reshape(2 * pairs, LINES, W3, C3)
    result = jnp.pad(result, ((0, 0), (0, H3 - LINES), (0, 0), (0, 0)))
    result = jnp.where(flips, result.transpose(0, 2, 1, 3), result)
    result = result.reshape(1, 1, 2 * pairs, H3, W3, 1, C3)
    result, vectors_in[0] = lax.optimization_barrier((result, vectors_in[0]))
    result = result.transpose(0, 1, 2, 5, 3, 4, 6).reshape(out_grad.shape)
    pixel_back, pieces[2] = lax.optimization_barrier((pixel_back, pieces[2]))
    returned = share_out(pixel_back, "tile")
    own, *parts = fold_tile(spot, pieces, vectors_in, extra, batch_count)
    parts = [
        lax.ppermute(part, "batch", [(i, (i + k + 1) % batch_count) for i in range(batch_count)])
        for k, part in enumerate(parts)
    ]
    quarter = fold_batch(spot, [own] + parts, owned, tile_count)
    returned, quarter = lax.optimization_barrier((returned, quarter))
    quarters = [quarter] + [
        lax.ppermute(quarter, "batch", [(i, (i + k) % batch_count) for i in range(batch_count)])
        for k in range(1, batch_count)
    ]
    norm = square_sum(spot, quarters)
    if paired:
        norm = norm + swap(norm, 1)
        norms = [norm] + [swap(norm, 2 * k) for k in range(1, tile_count // 2)]
        norms += [jnp.zeros_like(norm)] * (4 - len(norms))
    else:
        norm = jnp.broadcast_to(norm[None], (tile_count,) + norm.shape)
        norms = [jnp.sum(share_out(norm, "tile"), axis=0)]
        norms += [jnp.zeros_like(norms[0])] * 3
    returned = returned.astype(f32).transpose(1, 2, 0, 3)
    returned, norms[-1] = lax.optimization_barrier((returned, norms[-1]))
    returned = returned.transpose(2, 0, 1, 3).reshape(pixels.shape)
    block_grad, left_new, right_new, master_new, weight_copy, whole_vector, clip = update(
        spot, norms, quarters, extra, master, left_stat, right_stat, left_root, right_root
    )
    clip_norm = clip[0, 0]
    share = vectors.shape[0] // tile_count
    whole_vector = whole_vector.reshape(-1)
    vec_grad = lax.dynamic_slice_in_dim(whole_vector, tile_place * share, share, 0)
    vec_moment = moment + vec_grad * vec_grad
    own_vectors = lax.dynamic_slice_in_dim(vectors, tile_place * share, share, 0)
    vec_new = own_vectors - rate_vector * vec_grad / (jnp.sqrt(vec_moment) + eps_adagrad)
    return (
        result,
        returned,
        clip_norm,
        block_grad,
        left_new,
        right_new,
        master_new,
        weight_copy,
        vec_grad,
        vec_moment,
        vec_new,
    )


def solution(mesh):
    placed = (
        P("batch", "tile", None, None, None, None),
        P("batch"),
        P(),
        P("batch", "tile", None, None, None, None, None),
        P("tile", None, None),
        P("tile", None, None),
        P("tile", None, None),
        P("tile", None, None),
        P("tile", None, None),
        P(),
        P("tile"),
    )
    return jax.shard_map(
        on_device,
        mesh=mesh,
        in_specs=placed,
        out_specs=(
            P("batch", "tile", None, None, None, None, None),
            P("batch", "tile", None, None, None, None),
            P(),
            P("tile", None, None),
            P("tile", None, None),
            P("tile", None, None),
            P("tile", None, None),
            P("tile", None, None),
            P("tile"),
            P("tile"),
            P("tile"),
        ),
        check_vma=False,
    )
```

```python
import functools

import jax
import jax.numpy as jnp
from jax import lax
from jax.experimental import pallas as pl
from jax.experimental.layout import Layout, with_layout_constraint
from jax.experimental.pallas import tpu as pltpu
from jax.sharding import PartitionSpec as P

C2 = 128
HID2 = 512
C3 = 320
HID3 = 1280
CH = 36
CW = 36
STRIPS = 4
BS = 64
SR = CH // STRIPS
H3 = CH // 2
W3 = CW // 2
LONG = 7 * CH // 9
LINES = LONG // 2
WIDE = 384
LINE = 40
AREA = LINES * LINE
STEP = 2 * LINE
STEPS = AREA // STEP
HALF = BS // 2

eps_norm = 1e-05
clip_limit = 1.0
rate_matrix = 0.3
rate_vector = 0.3
eps_adagrad = 1e-08
f32 = jnp.float32
bf16 = jnp.bfloat16

SHAPES = [(C2, HID2), (HID2, C2), (9 * C2, C3), (C3, HID3), (HID3, C3)]
USED = sum(rows // BS * (cols // BS) for rows, cols in SHAPES)
VEC_ROWS = (6 * C2 + HID2 + C2 + C3 + 6 * C3 + HID3 + C3) // 128


VEC_BLOCKS = -(-VEC_ROWS // HALF)


def extra_of(owned, groups):
    return VEC_BLOCKS + -(owned + VEC_BLOCKS) % groups


def product(left, right):
    return jnp.dot(left, right, preferred_element_type=f32)


def product_nt(left, right):
    return lax.dot_general(left, right, (((1,), (1,)), ((), ())), preferred_element_type=f32)


def product_tn(left, right):
    return lax.dot_general(left, right, (((0,), (0,)), ((), ())), preferred_element_type=f32)


def gelu_pair(values):
    bell = jnp.exp2(values * values * (-0.5 * 1.4426950408889634))
    step = pl.reciprocal(1.0 + (0.3275911 * 0.7071067811865476) * jnp.abs(values), approx=True)
    tail = step * (
        0.5 * 0.254829592
        + step
        * (
            0.5 * -0.284496736
            + step
            * (0.5 * 1.421413741 + step * (0.5 * -1.453152027 + step * (0.5 * 1.061405429)))
        )
    )
    tail = tail * bell
    share = jnp.where(values >= 0.0, 1.0 - tail, tail)
    return (values * share, share + values * (bell * 0.3989422804014327))


def fold(values):
    chans = values.shape[-1]
    return jnp.sum(values.reshape(-1, 8, chans), axis=0)


def by_image(total):
    total = total + pltpu.roll(total, 4, 0)
    total = total + pltpu.roll(total, 2, 0)
    return jnp.sum(total, axis=1, keepdims=True)


def line(pattern):
    return jnp.concatenate([pattern] * (LINE // 8), axis=0)


def spread(pattern, chans):
    return jnp.broadcast_to(pattern, (8, chans))


def affine(values, factor, shift):
    tiles = values.reshape(-1, 8, values.shape[-1])
    return (tiles * factor + shift).reshape(values.shape)


def scaled(values, factor):
    tiles = values.reshape(-1, 8, values.shape[-1])
    return (tiles * factor).reshape(values.shape)


def from_left(values):
    return pltpu.roll(values, 2, 0)


def from_right(values):
    return pltpu.roll(values, values.shape[0] - 2, 0)


def rounded(values):
    return values.astype(bf16).astype(f32)


def widen(values):
    return jnp.concatenate([values] * (WIDE // 128), axis=-1)


def norm_terms(total, square, count):
    mean = by_image(total) / count
    scaling = lax.rsqrt(by_image(square) / count - mean * mean + eps_norm)
    return (mean, scaling)


def sweep(visit, start):
    return lax.fori_loop(0, STEPS, visit, start, unroll=True)


def step_rows(k, lines=0):
    start = k * STEP + lines * LINE
    return pl.ds(start if isinstance(k, int) else pl.multiple_of(start, LINE), STEP)


def held_in(space, *arrays):
    return [pltpu.with_memory_space_constraint(array, space) for array in arrays]


VMEM_BLOCK = pl.BlockSpec(memory_space=pltpu.VMEM)
HBM = pl.BlockSpec(memory_space=pltpu.HBM)
SMEM = pl.BlockSpec(memory_space=pltpu.SMEM)


def roomy(mebibytes):
    return pltpu.CompilerParams(vmem_limit_bytes=mebibytes * 1024 * 1024)


class Geometry:
    def __init__(self, size_ref, pair):
        parity = lax.broadcasted_iota(jnp.int32, (8, 128), 0) % 2
        high, broad, turned = (
            jnp.where(parity == 0, size_ref[pair * 6 + n], size_ref[pair * 6 + 3 + n])
            for n in range(3)
        )
        self.high = high
        self.count_two = (high * broad * C2).astype(f32)[:, :1]
        self.high3 = (high + 1) // 2
        broad3 = (broad + 1) // 2
        self.count_three = (self.high3 * broad3 * C3).astype(f32)[:, :1]
        place = lax.broadcasted_iota(jnp.int32, (LINE, 128), 0) // 2
        inside = lax.broadcasted_iota(jnp.int32, (LINE, 128), 0) < 2 * W3
        self.reach = []
        self.col_share = []
        for pc in range(2):
            column = 2 * place + pc
            self.reach.append(jnp.where(inside & (column < line(broad)), line(high), 0))
            edge = (column == 0) | (column == line(broad) - 1)
            self.col_share.append(jnp.where(edge, 0.5, 1.0 / 3.0))
        self.reach3 = jnp.where(inside & (place < line(broad3)), line(self.high3), 0)
        edge3 = (place == 0) | (place == line(broad3) - 1)
        self.col_share3 = jnp.where(edge3, 0.5, 1.0 / 3.0)
        self.flipped = jnp.concatenate([turned] * (STEP // 8), axis=0) > 0

    def share(self, plane, k):
        pr, pc = plane // 2, plane % 2
        return self.lines(4 * k + pr, 2, self.reach[pc], self.col_share[pc], self.high)

    def share3(self, k):
        return self.lines(2 * k, 1, self.reach3, self.col_share3, self.high3)

    def lines(self, row, stride, reach, col_share, height):
        parts = []
        for n in range(2):
            here = row + stride * n
            row_share = jnp.where((here == 0) | (here == height - 1), 0.5, 1.0 / 3.0)
            parts.append(jnp.where(here < reach, line(row_share) * col_share, 0.0))
        return jnp.concatenate(parts, axis=0)


def strip_place(pair, spot, strip_count):
    return lax.rem(pair * 8 + strip_count - 2 + spot, strip_count)


def each_image(size_ref, pair, visit):
    for image in range(2):
        way = size_ref[pair * 6 + 3 * image + 2]
        for flat in (True, False):

            @pl.when(way == (0 if flat else 1))
            def _():
                def one(r, carry):
                    for pr in range(2):
                        for pc in range(2):
                            line_place = pl.ds(r * LINE + image, W3, stride=2)
                            if flat:
                                there = pl.ds((2 * r + pr) * LINE + pc, W3, stride=2)
                            else:
                                there = pl.ds(pc * LINE + 2 * r + pr, W3, stride=2 * LINE)
                            visit(image, pr * 2 + pc, line_place, there)
                    return carry

                lax.fori_loop(0, LINES, one, 0)


def row_windows(col_ref, pc, k):
    both = col_ref[pc, step_rows(k, 1)] + col_ref[2 + pc, step_rows(k, 1)]
    return (both + col_ref[2 + pc, step_rows(k)], both + col_ref[pc, step_rows(k, 2)])


def put_col_windows(col_ref, pr, k, even, odd):
    both = even + odd
    col_ref[pr * 2, step_rows(k, 1)] = both + from_left(odd)
    col_ref[pr * 2 + 1, step_rows(k, 1)] = both + from_right(even)


def clear_edges(col_ref):
    zero_line = jnp.zeros((LINE, C2), f32)
    for plane in range(4):
        col_ref[plane, 0:LINE] = zero_line
        col_ref[plane, AREA + LINE : AREA + 2 * LINE] = zero_line


def entry_kernel(
    pairs,
    strip_count,
    size_ref,
    strips_ref,
    vec_two_ref,
    x_out,
    inv_out,
    pool_out,
    mix_out,
    stat_out,
    image_ref,
    col_ref,
):
    pair = pl.program_id(0) if pairs > 1 else 0
    x_ref, inv_ref, pool_ref, mix_ref = (ref.at[0] for ref in (x_out, inv_out, pool_out, mix_out))
    shape = Geometry(size_ref, pair)
    gain1, bias1, scale1 = (vec_two_ref[n : n + 1] for n in range(3))
    clear_edges(col_ref)

    def to_rows(within, carry):
        for spot in range(2 * STRIPS):
            image, strip = spot // STRIPS, spot % STRIPS
            start = pl.multiple_of((strip * SR + within) * LINE, LINE)
            source = strip_place(pair, spot, strip_count)
            image_ref[image, pl.ds(start, CW)] = strips_ref[source, within].astype(f32)
        return carry

    lax.fori_loop(0, SR, to_rows, 0)

    def take_in(image, plane, line_place, there):
        x_ref[plane, line_place] = image_ref[image, there]

    each_image(size_ref, pair, take_in)

    def arrange(k, carry):
        total, square = carry
        rows = step_rows(k)
        for plane in range(4):
            share = shape.share(plane, k)
            inv_ref[plane, rows] = share
            values = jnp.where(share > 0.0, x_ref[plane, rows], 0.0)
            x_ref[plane, rows] = values
            total = total + fold(values)
            square = square + fold(values * values)
        return (total, square)

    nothing = jnp.zeros((8, C2), f32)
    total, square = sweep(arrange, (nothing, nothing))
    mean1, scaling1 = norm_terms(total, square, shape.count_two)
    factor1 = scaling1 * gain1
    shift1 = bias1 - mean1 * scaling1 * gain1

    def window_cols(k, carry):
        rows = step_rows(k)
        for pr in range(2):
            masked = []
            for pc in range(2):
                plane = pr * 2 + pc
                normal = rounded(affine(x_ref[plane, rows], factor1, shift1))
                masked.append(jnp.where(inv_ref[plane, rows] > 0.0, normal, 0.0))
            put_col_windows(col_ref, pr, k, *masked)
        return carry

    sweep(window_cols, 0)

    def mix(k, carry):
        total, square = carry
        rows = step_rows(k)
        for pc in range(2):
            windows = row_windows(col_ref, pc, k)
            for pr in range(2):
                plane = pr * 2 + pc
                values = x_ref[plane, rows]
                share = inv_ref[plane, rows]
                pooled = windows[pr] * share - rounded(affine(values, factor1, shift1))
                pooled = jnp.where(share > 0.0, pooled, 0.0)
                mixed = values + scale1 * pooled
                pool_ref[plane, rows] = pooled
                mix_ref[plane, rows] = mixed
                total = total + fold(mixed)
                square = square + fold(mixed * mixed)
        return (total, square)

    total, square = sweep(mix, (nothing, nothing))
    mean2, scaling2 = norm_terms(total, square, shape.count_two)
    for n, value in enumerate((mean1, scaling1, mean2, scaling2)):
        stat_out[0, n] = spread(value, 128)


def pair_specs(pairs, shapes, mode=None):
    if pairs == 1:
        return [VMEM_BLOCK] * len(shapes)
    return [
        pl.BlockSpec(
            (1,) + shape, lambda t, rank=len(shape): (t,) + (0,) * rank, pipeline_mode=mode
        )
        for shape in shapes
    ]


def whole_specs(pairs, shapes):
    if pairs == 1:
        return [VMEM_BLOCK] * len(shapes)
    return [
        pl.BlockSpec(
            shape,
            lambda t, rank=len(shape): (0,) * rank,
            pipeline_mode=pl.Buffered(1),
        )
        for shape in shapes
    ]


def pair_arrays(pairs, shapes, kinds):
    make = pltpu.VMEM if pairs == 1 else jax.ShapeDtypeStruct
    return [make((pairs,) + shape, kind) for shape, kind in zip(shapes, kinds)]


STATE = [(4, AREA, C2)] * 4 + [(4, 8, 128)]
BACK = [(4, AREA, C2)] * 2 + [(2, 8, 128)]


def run_entry(sizes, strips, vec_two):
    strip_count = strips.shape[0]
    pairs = strip_count // 8
    return pl.pallas_call(
        functools.partial(entry_kernel, pairs, strip_count),
        grid=() if pairs == 1 else (pairs,),
        in_specs=[SMEM] + whole_specs(pairs, [strips.shape, vec_two.shape]),
        out_specs=pair_specs(pairs, STATE),
        out_shape=pair_arrays(pairs, STATE, [f32] * 5),
        scratch_shapes=[
            pltpu.VMEM((2, CH * LINE, C2), f32),
            pltpu.VMEM((4, AREA + 2 * LINE, C2), f32),
        ],
        compiler_params=roomy(6 if pairs == 1 else 40),
        name="entry",
    )(sizes, strips, vec_two)


WEIGHTS = [(C2, HID2), (HID2, C2), (9 * C2, WIDE), (WIDE, HID3), (HID3, WIDE)]


def unpack_kernel(piece_count, slot_ref, *refs):
    piece_refs, refs = refs[:piece_count], refs[piece_count:]
    weights, gathered_ref = refs[:-1], refs[-1]
    count = piece_refs[0].shape[0]
    for n, ref in enumerate(piece_refs):
        gathered_ref[n * count : n * count + count] = ref[...]
    left_half = lax.broadcasted_iota(jnp.int32, (HALF, 128), 1) < BS
    offset = 0
    for (rows, cols), ref in zip(SHAPES, weights):
        wide = cols // BS
        for rb in range(rows // BS):
            for cb in range(0, wide, 2):
                number = offset + rb * wide + cb
                first = gathered_ref[slot_ref[number]]
                turned = pltpu.roll(first, BS, 1)
                if cb + 1 < wide:
                    second = gathered_ref[slot_ref[number + 1]]
                    top = jnp.where(left_half, first, pltpu.roll(second, BS, 1))
                    low = jnp.where(left_half, turned, second)
                else:
                    top = jnp.where(left_half, first, 0.0)
                    low = jnp.where(left_half, turned, 0.0)
                place = slice(cb * BS, cb * BS + 128)
                ref[rb * BS : rb * BS + HALF, place] = top
                ref[rb * BS + HALF : rb * BS + BS, place] = low
        offset += rows // BS * wide
    weights[3][C3:, :] = jnp.zeros((WIDE - C3, HID3), bf16)


def run_unpack(slot_of, pieces):
    slots = sum(piece.shape[0] for piece in pieces)
    return pl.pallas_call(
        functools.partial(unpack_kernel, len(pieces)),
        in_specs=[SMEM] + [VMEM_BLOCK] * len(pieces),
        out_specs=[VMEM_BLOCK] * 5,
        out_shape=[pltpu.VMEM(shape, bf16) for shape in WEIGHTS],
        scratch_shapes=[pltpu.VMEM((slots, HALF, 128), bf16)],
        compiler_params=roomy(6),
        name="unpack",
    )(slot_of, *held_in(pltpu.VMEM, *pieces))


def main_kernel(
    pairs,
    strip_count,
    slots,
    near_place,
    far_place,
    size_ref,
    inv_in,
    mix_in,
    stat_in,
    goal_ref,
    vec_two_ref,
    vec_hid_two_ref,
    vec_three_ref,
    vec_hid_three_ref,
    w1_ref,
    w2_ref,
    we_ref,
    w3_ref,
    w4_ref,
    result_ref,
    zed_out,
    dx_out,
    mean_out,
    near_ref,
    far_ref,
    flat_ref,
    zed_ref,
    hid_ref,
    u_ref,
    g_ref,
    h_ref,
    dy_ref,
    patch_ref,
    dpatch_ref,
    inv3_ref,
    e_ref,
    col3_ref,
    pool3_ref,
    mix3_ref,
    dx3_ref,
    hid3_ref,
    dhid3_ref,
    u3_ref,
    g3_ref,
    h3_ref,
    dy3_ref,
    dpre_ref,
    gw1_ref,
    gw2_ref,
    gwe_ref,
    gw3_ref,
    gw4_ref,
    acc_two,
    acc_hid_two,
    acc_three,
    acc_hid_three,
):
    pair = pl.program_id(0) if pairs > 1 else 0
    grads = [gw1_ref, gw2_ref, gwe_ref, gw3_ref, gw4_ref]
    inv_ref, mix_ref, stat_ref = (ref.at[0] for ref in (inv_in, mix_in, stat_in))
    back_ref, dx_ref = zed_out.at[0], dx_out.at[0]
    left_half = lax.broadcasted_iota(jnp.int32, (HALF, 128), 1) < BS

    def at_pair(number, act):
        if pairs == 1:
            act()
        else:
            pl.when(pair == number)(act)

    def begin():
        acc_two[...] = jnp.zeros(acc_two.shape, f32)
        acc_hid_two[...] = jnp.zeros(acc_hid_two.shape, f32)
        acc_three[...] = jnp.zeros(acc_three.shape, f32)
        acc_hid_three[...] = jnp.zeros(acc_hid_three.shape, f32)

    at_pair(0, begin)
    shape = Geometry(size_ref, pair)
    count_two, count_three, flipped = shape.count_two, shape.count_three, shape.flipped
    nothing = jnp.zeros((8, C2), f32)
    nothing3 = jnp.zeros((8, WIDE), f32)
    gain2, bias2, scale2, out_bias = (vec_two_ref[n : n + 1] for n in range(3, 7))
    embed_bias, gain3, bias3, scale3 = (vec_three_ref[n : n + 1] for n in range(4))
    gain4, bias4, scale4, out_bias3 = (vec_three_ref[n : n + 1] for n in range(4, 8))
    mean2, scaling2 = stat_ref[2], stat_ref[3]
    factor2 = scaling2 * gain2
    shift2 = bias2 - mean2 * scaling2 * gain2
    for plane in range(4):
        zed_ref[plane, 0:LINE] = jnp.zeros((LINE, C2), f32)
    col3_ref[0:LINE] = jnp.zeros((LINE, WIDE), f32)
    col3_ref[AREA + LINE : AREA + 2 * LINE] = jnp.zeros((LINE, WIDE), f32)

    def put_block(number, block):
        near_ref[near_place[number]] = block
        far_ref[far_place[number]] = block

    def pack_blocks(matrices):
        offsets = [0]
        for rows, cols in SHAPES:
            offsets.append(offsets[-1] + rows // BS * (cols // BS))
        for which in matrices:
            (rows, cols), ref = SHAPES[which], grads[which]
            wide = cols // BS
            for rb in range(rows // BS):
                for cb in range(0, wide, 2):
                    number = offsets[which] + rb * wide + cb
                    at = slice(cb * BS, cb * BS + 128)
                    top = ref[rb * BS : rb * BS + HALF, at].astype(bf16)
                    low = ref[rb * BS + HALF : rb * BS + BS, at].astype(bf16)
                    put_block(number, jnp.where(left_half, top, pltpu.roll(low, BS, 1)))
                    if cb + 1 < wide:
                        put_block(number + 1, jnp.where(left_half, pltpu.roll(top, BS, 1), low))

    def plane_rows(plane):
        return slice(plane * AREA, plane * AREA + AREA)

    def begin_plane(plane):
        low = affine(mix_ref[plane], factor2, shift2).astype(bf16)
        h_ref[plane_rows(plane)] = low
        hid_ref[plane % 2] = product(low, w1_ref[...])

    begin_plane(0)
    for plane in range(4):
        if plane < 3:
            begin_plane(plane + 1)
        for k in range(STEPS):
            rows = step_rows(k)
            flat = slice(plane * AREA + k * STEP, plane * AREA + k * STEP + STEP)
            for at in range(0, HID2, 128):
                lanes = slice(at, at + 128)
                active, slope = gelu_pair(hid_ref[plane % 2, rows, lanes] + vec_hid_two_ref[:, lanes])
                u_ref[flat, lanes] = active.astype(bf16)
                g_ref[flat, lanes] = slope.astype(bf16)
        out = product(u_ref[plane_rows(plane)], w2_ref[...]) + out_bias
        zed = jnp.where(inv_ref[plane] > 0.0, mix_ref[plane] + scale2 * out, 0.0)
        zed_ref[plane, LINE : LINE + AREA] = rounded(zed)

    def patches(k, carry):
        rows = step_rows(k)
        taps = []
        for ky in range(3):
            pr = (0 if ky == 1 else 1) * 2
            source = step_rows(k, 0 if ky == 0 else 1)
            even = zed_ref[pr, source]
            odd = zed_ref[pr + 1, source]
            taps.append((from_left(odd), even, odd))
        for ky in range(3):
            for kx in range(3):
                at = (3 * ky + kx) * C2
                tap = taps[ky][kx]
                if ky != kx:
                    tap = jnp.where(flipped, taps[kx][ky], tap)
                patch_ref[rows, at : at + C2] = tap.astype(bf16)
        return carry

    sweep(patches, 0)
    e_ref[...] = product(patch_ref[...], we_ref[...])

    def embed(k, carry):
        total, square = carry
        rows = step_rows(k)
        share = shape.share3(k)
        inv3_ref[rows] = share
        out = jnp.where(widen(share) > 0.0, e_ref[rows] + embed_bias, 0.0)
        e_ref[rows] = out
        return (total + fold(out), square + fold(out * out))

    total, square = sweep(embed, (nothing3, nothing3))
    mean3, scaling3 = norm_terms(total, square, count_three)
    factor3 = scaling3 * gain3
    shift3 = bias3 - mean3 * scaling3 * gain3

    def window_cols3(k, carry):
        rows = step_rows(k)
        normal = rounded(affine(e_ref[rows], factor3, shift3))
        masked = jnp.where(widen(inv3_ref[rows]) > 0.0, normal, 0.0)
        col3_ref[step_rows(k, 1)] = masked + from_left(masked) + from_right(masked)
        return carry

    sweep(window_cols3, 0)

    def row_windows3(k):
        return col3_ref[step_rows(k)] + col3_ref[step_rows(k, 1)] + col3_ref[step_rows(k, 2)]

    def mix3(k, carry):
        total, square = carry
        rows = step_rows(k)
        values = e_ref[rows]
        share = widen(inv3_ref[rows])
        pooled = row_windows3(k) * share - rounded(affine(values, factor3, shift3))
        pooled = jnp.where(share > 0.0, pooled, 0.0)
        mixed = values + scale3 * pooled
        pool3_ref[rows] = pooled
        mix3_ref[rows] = mixed
        return (total + fold(mixed), square + fold(mixed * mixed))

    total, square = sweep(mix3, (nothing3, nothing3))
    mean4, scaling4 = norm_terms(total, square, count_three)
    factor4 = scaling4 * gain4
    shift4 = bias4 - mean4 * scaling4 * gain4
    normal4 = (spread(scaling4, WIDE), spread(-mean4 * scaling4, WIDE))

    def prepare3(k, d_bias):
        rows = step_rows(k)
        h3_ref[rows] = affine(mix3_ref[rows], factor4, shift4).astype(bf16)
        goal = goal_ref[0, rows].astype(f32)
        goal = jnp.where(widen(inv3_ref[rows]) > 0.0, goal, 0.0)
        low_goal = (scale4 * goal).astype(bf16)
        dy3_ref[rows] = low_goal
        return d_bias + fold(low_goal.astype(f32))

    acc_three[7] += sweep(prepare3, nothing3)

    def keep(ref, value, place=slice(None)):
        if pairs == 1:
            ref[place] = value.astype(ref.dtype)
        else:

            @pl.when(pair == 0)
            def _():
                ref[place] = value

            @pl.when(pair > 0)
            def _():
                ref[place] += value

    def begin_chunk(at):
        lanes = slice(at, at + 256)
        hid3_ref[:, lanes] = product(h3_ref[...], w3_ref[:, lanes])
        dhid3_ref[:, lanes] = product_nt(dy3_ref[...], w4_ref[lanes])

    begin_chunk(0)
    for at in range(0, HID3, 256):
        if at + 256 < HID3:
            begin_chunk(at + 256)
        for lane in (at, at + 128):
            lanes = slice(lane, lane + 128)
            total = nothing
            for k in range(STEPS):
                rows = step_rows(k)
                active, slope = gelu_pair(hid3_ref[rows, lanes] + vec_hid_three_ref[:, lanes])
                u3_ref[rows, lanes] = active.astype(bf16)
                low = (slope * dhid3_ref[rows, lanes]).astype(bf16)
                g3_ref[rows, lanes] = low
                total = total + fold(low.astype(f32))
            acc_hid_three[:, lanes] += total
        lanes = slice(at, at + 256)
        out = product(u3_ref[:, lanes], w4_ref[lanes])
        d_low = product_nt(g3_ref[:, lanes], w3_ref[:, lanes])
        result_ref[0] = out if at == 0 else result_ref[0] + out
        dx3_ref[...] = d_low if at == 0 else dx3_ref[...] + d_low
        keep(gw3_ref, product_tn(h3_ref[...], g3_ref[:, lanes]), (slice(None), lanes))
        keep(gw4_ref, product_tn(u3_ref[:, lanes], dy3_ref[...]), lanes)

    def finish3(k, carry):
        d_scale, d_shift, d_gain = carry
        rows = step_rows(k)
        valid = widen(inv3_ref[rows]) > 0.0
        mixed = mix3_ref[rows]
        out = jnp.where(valid, result_ref[0, rows] + out_bias3, 0.0)
        result_ref[0, rows] = mixed + scale4 * out
        d_scale = d_scale + fold(out * goal_ref[0, rows].astype(f32))
        d_low = dx3_ref[rows]
        normal = affine(mixed, *normal4)
        return (d_scale, d_shift + fold(d_low), d_gain + fold(d_low * normal))

    d_scale, d_shift, d_gain = sweep(finish3, (nothing3, nothing3, nothing3))
    acc_three[6] += d_scale
    acc_three[5] += d_shift
    acc_three[4] += d_gain
    mean_shift = by_image(d_shift * gain4) / count_three
    mean_gain = by_image(d_gain * gain4) / count_three
    back_gain4 = scaling4 * gain4
    back_mean4 = spread(-scaling4 * mean_shift, WIDE)
    back_normal4 = spread(scaling4 * mean_gain, WIDE)

    def unmix3(k, d_scale):
        rows = step_rows(k)
        share = widen(inv3_ref[rows])
        valid = share > 0.0
        normal = affine(mix3_ref[rows], *normal4)
        back = affine(dx3_ref[rows], back_gain4, back_mean4) - scaled(normal, back_normal4)
        d_mixed = jnp.where(valid, back + goal_ref[0, rows].astype(f32), 0.0)
        dx3_ref[rows] = d_mixed
        d_scale = d_scale + fold(pool3_ref[rows] * d_mixed)
        weighted = scale3 * d_mixed * share
        col3_ref[step_rows(k, 1)] = weighted + from_left(weighted) + from_right(weighted)
        return d_scale

    acc_three[3] += sweep(unmix3, nothing3)
    normal3 = (spread(scaling3, WIDE), spread(-mean3 * scaling3, WIDE))

    def unpool3(k, carry):
        d_shift, d_gain = carry
        rows = step_rows(k)
        valid = widen(inv3_ref[rows]) > 0.0
        d_normal = jnp.where(valid, row_windows3(k) - scale3 * dx3_ref[rows], 0.0)
        pool3_ref[rows] = d_normal
        normal = affine(e_ref[rows], *normal3)
        return (d_shift + fold(d_normal), d_gain + fold(d_normal * normal))

    d_shift, d_gain = sweep(unpool3, (nothing3, nothing3))
    acc_three[2] += d_shift
    acc_three[1] += d_gain
    mean_shift = by_image(d_shift * gain3) / count_three
    mean_gain = by_image(d_gain * gain3) / count_three
    back_gain3 = scaling3 * gain3
    back_mean3 = spread(-scaling3 * mean_shift, WIDE)
    back_normal3 = spread(scaling3 * mean_gain, WIDE)

    def unnorm3(k, d_bias):
        rows = step_rows(k)
        valid = widen(inv3_ref[rows]) > 0.0
        normal = affine(e_ref[rows], *normal3)
        back = affine(pool3_ref[rows], back_gain3, back_mean3) - scaled(normal, back_normal3)
        low = jnp.where(valid, dx3_ref[rows] + back, 0.0).astype(bf16)
        dpre_ref[rows] = low
        return d_bias + fold(low.astype(f32))

    acc_three[0] += sweep(unnorm3, nothing3)
    keep(gwe_ref, product_tn(patch_ref[...], dpre_ref[...]))
    dpatch_ref[0:AREA] = product_nt(dpre_ref[...], we_ref[...])
    dpatch_ref[AREA : AREA + LINE] = jnp.zeros((LINE, 9 * C2), f32)

    def gather_back(k, carry):
        rows = step_rows(k)

        def tap(ky, kx, source):
            at = (3 * ky + kx) * C2
            value = dpatch_ref[source, at : at + C2]
            if ky != kx:
                at = (3 * kx + ky) * C2
                value = jnp.where(flipped, dpatch_ref[source, at : at + C2], value)
            return value

        sources = []
        for ky in range(3):
            source = step_rows(k, 1 if ky == 0 else 0)
            sources.append(
                (tap(ky, 1, source), tap(ky, 2, source) + from_right(tap(ky, 0, source)))
            )
        for pc in range(2):
            for pr, value in ((0, sources[1][pc]), (1, sources[2][pc] + sources[0][pc])):
                plane = pr * 2 + pc
                valid = inv_ref[plane, rows] > 0.0
                back_ref[plane, rows] = jnp.where(valid, rounded(value), 0.0)
        return carry

    sweep(gather_back, 0)

    if pairs == 1:
        pack_blocks(range(2, 5))

    normal2 = (spread(scaling2, C2), spread(-mean2 * scaling2, C2))

    def begin_back(plane):
        low_goal = (scale2 * back_ref[plane]).astype(bf16)
        dy_ref[plane_rows(plane)] = low_goal
        hid_ref[plane % 2] = product_nt(low_goal, w2_ref[...])
        return fold(low_goal.astype(f32))

    d_out_bias = begin_back(0)
    d_shift, d_gain = nothing, nothing
    sums = [nothing] * (HID2 // 128)
    new_gw1, new_gw2 = None, None
    for plane in range(4):
        if plane < 3:
            d_out_bias = d_out_bias + begin_back(plane + 1)
        for k in range(STEPS):
            rows = step_rows(k)
            part = slice(plane * AREA + k * STEP, plane * AREA + k * STEP + STEP)
            for n, at in enumerate(range(0, HID2, 128)):
                lanes = slice(at, at + 128)
                low = g_ref[part, lanes].astype(f32) * hid_ref[plane % 2, rows, lanes]
                low = low.astype(bf16)
                g_ref[part, lanes] = low
                sums[n] = sums[n] + fold(low.astype(f32))
        flat = plane_rows(plane)
        d_low = product_nt(g_ref[flat], w1_ref[...])
        dx_ref[plane] = d_low
        d_shift = d_shift + fold(d_low)
        d_gain = d_gain + fold(d_low * affine(mix_ref[plane], *normal2))
        part_gw1 = product_tn(h_ref[flat], g_ref[flat])
        part_gw2 = product_tn(dy_ref[flat], u_ref[flat])
        new_gw1 = part_gw1 if plane == 0 else new_gw1 + part_gw1
        new_gw2 = part_gw2 if plane == 0 else new_gw2 + part_gw2
    new_gw2 = new_gw2.T
    for n, value in enumerate(sums):
        acc_hid_two[:, n * 128 : n * 128 + 128] += value
    acc_two[6] += d_out_bias
    acc_two[4] += d_shift
    acc_two[3] += d_gain
    mean_out[0, 0] = spread(by_image(d_shift * gain2) / count_two, 128)
    mean_out[0, 1] = spread(by_image(d_gain * gain2) / count_two, 128)
    keep(gw1_ref, new_gw1)
    keep(gw2_ref, new_gw2)
    d_scale = fold(w2_ref[...].astype(f32) * new_gw2) + out_bias * d_out_bias
    acc_two[5] += d_scale / scale2

    def finish():
        if pairs > 1:
            pack_blocks(range(5))
        else:
            pack_blocks(range(2))

        def filler(number, carry):
            put_block(number, jnp.zeros((HALF, 128), bf16))
            return carry

        lax.fori_loop(USED, slots, filler, 0)

        flat_ref[...] = jnp.zeros(flat_ref.shape, f32)

        def put(at, total, length):
            if at % 128:
                room = jnp.zeros((8, 128), f32)
                if total.shape[1] < length + BS:
                    total = jnp.concatenate([total, room], axis=1)
                total = pltpu.roll(total, BS, 1)
            whole = jnp.sum(total, axis=0, keepdims=True)
            done = -(at % 128)
            row = at // 128
            lane = 0
            while done < length:
                first = max(0, -done)
                last = min(128, length - done)
                flat_ref[row : row + 1, first:last] = whole[:, lane + first : lane + last]
                done += 128
                lane += 128
                row += 1

        at = 3 * C2
        for n in range(3, 6):
            put(at, acc_two[n], C2)
            at += C2
        put(at, acc_hid_two[...], HID2)
        at += HID2
        put(at, acc_two[6], C2)
        at += C2
        for n in range(7):
            put(at, acc_three[n], C3)
            at += C3
        put(at, acc_hid_three[...], HID3)
        at += HID3
        put(at, acc_three[7], C3)

    at_pair(pairs - 1, finish)


def run_main(places, sizes, state, goal, vectors, weights, strip_count):
    pairs = goal.shape[0]
    slots = places[0].shape[0]
    half = slots // 2 + 1
    if pairs == 1:
        state = held_in(pltpu.VMEM, *state)
    weights = held_in(pltpu.VMEM, *weights)
    _, inv, _, mix, stat = state
    state_shapes = [STATE[1], STATE[3], STATE[4]]
    grad_kind = bf16 if pairs == 1 else f32
    wide_f32 = pltpu.VMEM((AREA, WIDE), f32)
    wide_bf16 = pltpu.VMEM((AREA, WIDE), bf16)
    scratch = [
        pltpu.VMEM((4, AREA + LINE, C2), f32),
        pltpu.VMEM((2, AREA, HID2), f32),
        pltpu.VMEM((4 * AREA, HID2), bf16),
        pltpu.VMEM((4 * AREA, HID2), bf16),
        pltpu.VMEM((4 * AREA, C2), bf16),
        pltpu.VMEM((4 * AREA, C2), bf16),
        pltpu.VMEM((AREA, 9 * C2), bf16),
        pltpu.VMEM((AREA + LINE, 9 * C2), f32),
        pltpu.VMEM((AREA, 128), f32),
        wide_f32,
        pltpu.VMEM((AREA + 2 * LINE, WIDE), f32),
        wide_f32,
        wide_f32,
        wide_f32,
        pltpu.VMEM((AREA, HID3), f32),
        pltpu.VMEM((AREA, HID3), f32),
        pltpu.VMEM((AREA, HID3), bf16),
        pltpu.VMEM((AREA, HID3), bf16),
        wide_bf16,
        wide_bf16,
        wide_bf16,
        pltpu.VMEM((C2, HID2), grad_kind),
        pltpu.VMEM((HID2, C2), grad_kind),
        pltpu.VMEM((9 * C2, WIDE), grad_kind),
        pltpu.VMEM((WIDE, HID3), grad_kind),
        pltpu.VMEM((HID3, WIDE), grad_kind),
        pltpu.VMEM((7, 8, C2), f32),
        pltpu.VMEM((8, HID2), f32),
        pltpu.VMEM((8, 8, WIDE), f32),
        pltpu.VMEM((8, HID3), f32),
    ]
    out_shapes = [(half, HALF, 128), (half, HALF, 128), (VEC_BLOCKS * HALF, 128)]
    make = pltpu.VMEM if pairs == 1 else jax.ShapeDtypeStruct
    return pl.pallas_call(
        functools.partial(main_kernel, pairs, strip_count, slots),
        grid=() if pairs == 1 else (pairs,),
        in_specs=[SMEM] * 3
        + pair_specs(pairs, state_shapes + [goal.shape[1:]], pl.Buffered(1))
        + whole_specs(pairs, [vector.shape for vector in vectors])
        + [VMEM_BLOCK] * 5,
        out_specs=pair_specs(pairs, [(AREA, WIDE)] + BACK) + whole_specs(pairs, out_shapes),
        out_shape=pair_arrays(pairs, [(AREA, WIDE)] + BACK, [f32] * 4)
        + [make(shape, kind) for shape, kind in zip(out_shapes, (bf16, bf16, f32))],
        scratch_shapes=scratch,
        compiler_params=pltpu.CompilerParams(
            vmem_limit_bytes=(40 if pairs == 1 else 56) * 1024 * 1024,
            fuse_transposed_lhs_in_matmul=True,
        ),
        name="blocks",
    )(*places, sizes, inv, mix, stat, goal, *vectors, *weights)


def exit_kernel(
    pairs,
    strip_count,
    size_ref,
    x_in,
    inv_in,
    pool_in,
    mix_in,
    stat_in,
    zed_in,
    dx_in,
    mean_in,
    flat_ref,
    vec_two_ref,
    payload_hbm,
    vector_ref,
    payload_ref,
    image_ref,
    col_ref,
    dx_ref,
    back_ref,
    acc_ref,
    sem,
):
    pair = pl.program_id(0) if pairs > 1 else 0
    x_ref, inv_ref, pool_ref, mix_ref, stat_ref, zed_ref, low_ref, mean_ref = (
        ref.at[0] for ref in (x_in, inv_in, pool_in, mix_in, stat_in, zed_in, dx_in, mean_in)
    )
    shape = Geometry(size_ref, pair)
    count_two = shape.count_two
    gain1, bias1, scale1, gain2 = (vec_two_ref[n : n + 1] for n in range(4))
    mean1, scaling1, mean2, scaling2 = (stat_ref[n] for n in range(4))
    normal2 = (scaling2, -mean2 * scaling2)
    clear_edges(col_ref)
    nothing = jnp.zeros((8, C2), f32)
    back_gain2 = scaling2 * gain2
    back_mean2 = -scaling2 * mean_ref[0]
    back_normal2 = scaling2 * mean_ref[1]

    if pairs > 1:

        @pl.when(pair == 0)
        def _():
            acc_ref[...] = jnp.zeros(acc_ref.shape, f32)

    def add_up(n, total):
        acc_ref[n] = total if pairs == 1 else acc_ref[n] + total

    def unmix(k, d_scale):
        rows = step_rows(k)
        for pr in range(2):
            weighted = []
            for pc in range(2):
                plane = pr * 2 + pc
                share = inv_ref[plane, rows]
                normal = affine(mix_ref[plane, rows], *normal2)
                back = affine(low_ref[plane, rows], back_gain2, back_mean2)
                back = back - scaled(normal, back_normal2)
                d_mixed = jnp.where(share > 0.0, zed_ref[plane, rows] + back, 0.0)
                dx_ref[plane, rows] = d_mixed
                d_scale = d_scale + fold(pool_ref[plane, rows] * d_mixed)
                weighted.append(scale1 * d_mixed * share)
            put_col_windows(col_ref, pr, k, *weighted)
        return d_scale

    add_up(2, sweep(unmix, nothing))
    normal1 = (spread(scaling1, C2), spread(-mean1 * scaling1, C2))

    def unpool(k, carry):
        d_shift, d_gain = carry
        rows = step_rows(k)
        for pc in range(2):
            windows = row_windows(col_ref, pc, k)
            for pr in range(2):
                plane = pr * 2 + pc
                valid = inv_ref[plane, rows] > 0.0
                d_normal = windows[pr] - scale1 * dx_ref[plane, rows]
                d_normal = jnp.where(valid, d_normal, 0.0)
                back_ref[plane, rows] = d_normal
                normal = affine(x_ref[plane, rows], *normal1)
                d_shift = d_shift + fold(d_normal)
                d_gain = d_gain + fold(d_normal * normal)
        return (d_shift, d_gain)

    d_shift, d_gain = sweep(unpool, (nothing, nothing))
    add_up(1, d_shift)
    add_up(0, d_gain)
    mean_shift = by_image(d_shift * gain1) / count_two
    mean_gain = by_image(d_gain * gain1) / count_two
    back_gain1 = scaling1 * gain1
    back_mean1 = spread(-scaling1 * mean_shift, C2)
    back_normal1 = spread(scaling1 * mean_gain, C2)

    def unnorm(k, carry):
        rows = step_rows(k)
        for plane in range(4):
            normal = affine(x_ref[plane, rows], *normal1)
            back = affine(back_ref[plane, rows], back_gain1, back_mean1)
            back = back - scaled(normal, back_normal1)
            valid = inv_ref[plane, rows] > 0.0
            dx_ref[plane, rows] = jnp.where(valid, dx_ref[plane, rows] + back, 0.0)
        return carry

    sweep(unnorm, 0)

    def give_back(image, plane, line_place, there):
        image_ref[image, there] = dx_ref[plane, line_place]

    image_ref[...] = jnp.zeros(image_ref.shape, f32)
    each_image(size_ref, pair, give_back)

    def from_rows(within, carry):
        for spot in range(2 * STRIPS):
            image, strip = spot // STRIPS, spot % STRIPS
            start = pl.multiple_of((strip * SR + within) * LINE, LINE)
            target = strip_place(pair, spot, strip_count)
            payload_ref[target, within] = image_ref[image, pl.ds(start, CW)].astype(bf16)
        return carry

    lax.fori_loop(0, SR, from_rows, 0)

    def finish():
        copy = pltpu.make_async_copy(payload_ref, payload_hbm, sem)
        copy.start()
        vector_ref[...] = flat_ref[...]
        for n in range(3):
            vector_ref[n : n + 1] = jnp.sum(acc_ref[n], axis=0, keepdims=True)
        copy.wait()

    if pairs == 1:
        finish()
    else:
        pl.when(pair == pairs - 1)(finish)


def run_exit(sizes, state, back, flat, vec_two, strip_count):
    pairs = strip_count // 8
    payload = (strip_count, SR, CW, C2)
    make = pltpu.VMEM if pairs == 1 else jax.ShapeDtypeStruct
    plane_f32 = pltpu.VMEM((4, AREA, C2), f32)
    arrays = [*state, *back]
    if pairs == 1:
        arrays = held_in(pltpu.VMEM, *arrays)
    return pl.pallas_call(
        functools.partial(exit_kernel, pairs, strip_count),
        grid=() if pairs == 1 else (pairs,),
        in_specs=[SMEM]
        + pair_specs(pairs, STATE + BACK, pl.Buffered(1))
        + whole_specs(pairs, [flat.shape, vec_two.shape]),
        out_specs=[HBM] + whole_specs(pairs, [flat.shape]),
        out_shape=[pltpu.HBM(payload, bf16), make(flat.shape, f32)],
        scratch_shapes=[
            pltpu.VMEM(payload, bf16),
            pltpu.VMEM((2, CH * LINE, C2), f32),
            pltpu.VMEM((4, AREA + 2 * LINE, C2), f32),
            plane_f32,
            plane_f32,
            pltpu.VMEM((3, 8, C2), f32),
            pltpu.SemaphoreType.DMA,
        ],
        compiler_params=roomy(8 if pairs == 1 else 40),
        name="exit",
    )(sizes, *arrays, flat, vec_two)


def pack_kernel(master_ref, dense_ref):
    values = master_ref[...]
    dense_ref[...] = jnp.concatenate([values[:, :HALF], values[:, HALF:]], axis=2).astype(bf16)


def pack(master):
    owned = master.shape[0]
    return pl.pallas_call(
        pack_kernel,
        out_shape=jax.ShapeDtypeStruct((owned, HALF, 2 * BS), bf16),
        name="pack",
    )(master)


def fold_pair_kernel(near_ref, got_ref, own_ref, *part_refs):
    share = own_ref.shape[0]

    def one(n, carry):
        for k in range(len(part_refs) + 1):
            total = near_ref[k * share + n].astype(f32) + got_ref[k * share + n].astype(f32)
            if k == 0:
                own_ref[n] = total
            else:
                part_refs[k - 1][n] = total.astype(bf16)
        return carry

    lax.fori_loop(0, share, one, 0, unroll=4)


def fold_pair(near, got, groups):
    shape = ((near.shape[0] - 1) // groups,) + near.shape[1:]
    return pl.pallas_call(
        fold_pair_kernel,
        in_specs=[VMEM_BLOCK] * 2,
        out_specs=[VMEM_BLOCK] * groups,
        out_shape=[pltpu.VMEM(shape, f32)] + [pltpu.VMEM(shape, bf16)] * (groups - 1),
        compiler_params=roomy(4),
        name="fold_pair",
    )(*held_in(pltpu.VMEM, near, got))


def fold_tile_kernel(pieces, spot_ref, *refs):
    piece_refs, refs = refs[:pieces], refs[pieces:]
    vector_refs, refs = refs[:pieces], refs[pieces:]
    out_refs, sum_ref = refs[:-1], refs[-1]
    groups = len(out_refs)
    share = out_refs[0].shape[0]
    owned = piece_refs[0].shape[0]
    total = vector_refs[0][...]
    for ref in vector_refs[1:]:
        total = total + ref[...]
    for n in range(sum_ref.shape[0]):
        sum_ref[n] = jnp.zeros((HALF, 128), f32)
    for n in range(VEC_BLOCKS):
        sum_ref[n] = total[n * HALF : (n + 1) * HALF]

    def one(n, carry):
        for k, out_ref in enumerate(out_refs):
            number = lax.rem(spot_ref[0] + k, groups) * share + n
            block = jnp.minimum(number, owned - 1)
            total = piece_refs[0][block].astype(f32)
            for ref in piece_refs[1:]:
                total = total + ref[block].astype(f32)
            rest = sum_ref[jnp.maximum(number - owned, 0)]
            out_ref[n] = jnp.where(number < owned, total, rest).astype(out_ref.dtype)
        return carry

    lax.fori_loop(0, share, one, 0, unroll=share <= 16)


def fold_tile(spot, pieces, vectors, extra, groups):
    shape = ((pieces[0].shape[0] + extra) // groups,) + pieces[0].shape[1:]
    return pl.pallas_call(
        functools.partial(fold_tile_kernel, len(pieces)),
        in_specs=[SMEM] + [VMEM_BLOCK] * (len(pieces) + len(vectors)),
        out_specs=[VMEM_BLOCK] * groups,
        out_shape=[pltpu.VMEM(shape, f32)] + [pltpu.VMEM(shape, bf16)] * (groups - 1),
        scratch_shapes=[pltpu.VMEM((extra, HALF, 128), f32)],
        compiler_params=roomy(8),
        name="fold_tile",
    )(spot, *held_in(pltpu.VMEM, *pieces, *vectors))


def fold_batch_kernel(owned, vector_weight, spot_ref, *refs):
    part_refs, total_ref = refs[:-1], refs[-1]
    share = total_ref.shape[0] - 1
    square = jnp.zeros((8, 128), f32)
    for n in range(share):
        total = part_refs[0][n].astype(f32)
        for ref in part_refs[1:]:
            total = total + ref[n].astype(f32)
        total_ref[n] = total.astype(bf16)
        weight = jnp.where(spot_ref[0] * share + n < owned, 1.0, vector_weight)
        square = square + weight * fold(total * total)
    rest = 0.25 * jnp.sum(jnp.sum(square, axis=1, keepdims=True), axis=0, keepdims=True)
    row = lax.broadcasted_iota(jnp.int32, (HALF, 128), 0)
    block = jnp.zeros((HALF, 128), f32)
    for n in range(3):
        term = rounded(rest)
        block = jnp.where(row == n, term, block)
        rest = rest - term
    total_ref[share] = block.astype(bf16)


def fold_batch(spot, parts, owned, tile_count):
    shape = (parts[0].shape[0] + 1,) + parts[0].shape[1:]
    return pl.pallas_call(
        functools.partial(fold_batch_kernel, owned, 1.0 / tile_count),
        in_specs=[SMEM] + [VMEM_BLOCK] * len(parts),
        out_specs=VMEM_BLOCK,
        out_shape=pltpu.VMEM(shape, bf16),
        compiler_params=roomy(4),
        name="fold_batch",
    )(spot, *held_in(pltpu.VMEM, *parts))


def norm_kernel(spot_ref, *refs):
    quarters, sum_ref = refs[:-1], refs[-1]
    groups = len(quarters)
    share = quarters[0].shape[0] - 1
    total = jnp.zeros((1, 128), f32)
    for source in range(groups):
        turn = lax.rem(spot_ref[0] - source + groups, groups)
        terms = quarters[0][share].astype(f32)
        for k in range(1, groups):
            terms = jnp.where(turn == k, quarters[k][share].astype(f32), terms)
        total = total + 4.0 * (terms[0:1] + (terms[1:2] + terms[2:3]))
    sum_ref[...] = jnp.broadcast_to(total, sum_ref.shape)


def square_sum(spot, quarters):
    return pl.pallas_call(
        norm_kernel,
        in_specs=[SMEM] + [VMEM_BLOCK] * len(quarters),
        out_specs=VMEM_BLOCK,
        out_shape=pltpu.VMEM((8, 128), f32),
        compiler_params=roomy(4),
        name="norm",
    )(spot, *held_in(pltpu.VMEM, *quarters))


def update_kernel(owned, groups, spot_ref, *refs):
    norm_refs, quarters, refs = refs[:4], refs[4 : 4 + groups], refs[4 + groups :]
    stat_hbm, out_hbm, (vector_ref, clip_ref), refs = refs[:5], refs[5:10], refs[10:12], refs[12:]
    stat_refs, out_refs, (in_sem, out_sem) = refs[:5], refs[5:10], refs[10:]
    master_ref, left_stat_ref, right_stat_ref, left_root_ref, right_root_ref = stat_refs
    grad_ref, left_ref, right_ref, new_ref, copy_ref = out_refs
    share = quarters[0].shape[0] - 1
    spans = spans_of(owned)

    def copies_of(sources, targets, sems):
        return [
            [
                pltpu.make_async_copy(
                    source.at[pl.ds(*span)], target.at[pl.ds(*span)], sems.at[5 * n + k]
                )
                for k, (source, target) in enumerate(zip(sources, targets))
            ]
            for n, span in enumerate(spans)
        ]

    copies_in = copies_of(stat_hbm, stat_refs, in_sem)
    copies_out = copies_of(out_refs, out_hbm, out_sem)
    for copies in copies_in:
        for copy in copies:
            copy.start()
    total = [ref[0:1] for ref in norm_refs]
    norm = jnp.sqrt((total[0] + total[1]) + (total[2] + total[3]))
    factor = jnp.minimum(1.0, clip_limit / norm)
    left_half = lax.broadcasted_iota(jnp.int32, (HALF, 128), 1) < BS

    def summed(number):
        source = number // share
        local = number - source * share
        turn = lax.rem(spot_ref[0] - source + groups, groups)
        value = quarters[0][local].astype(f32)
        for k in range(1, groups):
            value = jnp.where(turn == k, quarters[k][local].astype(f32), value)
        return value * factor

    def side_by_side(first, count):
        sides = []
        for n in range(first, first + count, 2):
            dense = summed(n)
            turned = pltpu.roll(dense, BS, 1)
            if n + 1 < first + count:
                second = summed(n + 1)
                top = jnp.where(left_half, dense, pltpu.roll(second, BS, 1))
                low = jnp.where(left_half, turned, second)
                side = jnp.concatenate([top, low], axis=0)
                grad_ref[n + 1] = pltpu.roll(side, BS, 1)[:, :BS]
            else:
                side = jnp.concatenate([dense, turned], axis=0)[:, :BS]
            grad_ref[n] = side[:, :BS]
            sides.append(side.astype(bf16))
        return jnp.concatenate(sides, axis=1)

    def diagonal_of(count):
        order = (count * BS, count * BS)
        return lax.broadcasted_iota(jnp.int32, order, 0) // BS == (
            lax.broadcasted_iota(jnp.int32, order, 1) // BS
        )

    clip_ref[...] = norm
    for n in range(vector_ref.shape[0]):
        vector_ref[n] = summed(owned + n)
    for (first, length), arriving, leaving in zip(spans, copies_in, copies_out):
        parts = [(n, min(4, first + length - n)) for n in range(first, first + length, 4)]
        wides = [side_by_side(*part) for part in parts]
        tall = [
            jnp.where(diagonal_of(count), jnp.concatenate([wide] * count, axis=0), 0.0)
            for (_, count), wide in zip(parts, wides)
        ]
        lefts = [product_nt(one, wide) for one, wide in zip(tall, wides)]
        rights = [product_tn(wide, wide) for wide in wides]
        for copy in arriving:
            copy.wait()
        stepped = []
        for (start, count), wide in zip(parts, wides):
            roots = left_root_ref[pl.ds(start, count)].reshape(count * BS, BS).astype(bf16)
            stepped.append(product(roots, wide))
        for (start, count), left, right in zip(parts, lefts, rights):
            here = pl.ds(start, count)
            left_ref[here] = 0.5 * left_stat_ref[here] + 0.5 * left.reshape(count, BS, BS)
            for n in range(count):
                at = n // 2 * 128
                block = right[n * BS : n * BS + BS, at : min(at + 128, count * BS)]
                if n % 2:
                    block = pltpu.roll(block, BS, 1)
                right_ref[start + n] = 0.5 * right_stat_ref[start + n] + 0.5 * block[:, :BS]
        for (start, count), value in zip(parts, stepped):
            here = pl.ds(start, count)
            value = jnp.where(diagonal_of(count), value, 0.0).astype(bf16)
            roots = right_root_ref[here].reshape(count * BS, BS).astype(bf16)
            value = product(value, roots).reshape(count, BS, BS)
            new = master_ref[here] - rate_matrix * value
            new_ref[here] = new
            copy_ref[here] = new.astype(bf16)
        for copy in leaving:
            copy.start()
    for leaving in copies_out:
        for copy in leaving:
            copy.wait()


def spans_of(owned):
    spans = []
    first = 0
    while first < owned:
        length = min(8 if first == 0 else 12, owned - first)
        spans.append((first, length))
        first += length
    return spans


def update(spot, norms, quarters, extra, *stats):
    shape = stats[0].shape
    groups = len(quarters)
    types = [f32] * 4 + [bf16]
    steps = len(spans_of(shape[0]))
    return pl.pallas_call(
        functools.partial(update_kernel, shape[0], groups),
        in_specs=[SMEM] + [VMEM_BLOCK] * (groups + 4) + [HBM] * 5,
        out_specs=[HBM] * 5 + [VMEM_BLOCK] * 2,
        out_shape=[pltpu.HBM(shape, kind) for kind in types]
        + [
            jax.ShapeDtypeStruct((extra, HALF, 128), f32),
            jax.ShapeDtypeStruct((1, 128), f32),
        ],
        scratch_shapes=[pltpu.VMEM(shape, f32)] * 5
        + [pltpu.VMEM(shape, kind) for kind in types]
        + [
            pltpu.SemaphoreType.DMA((5 * steps,)),
            pltpu.SemaphoreType.DMA((5 * steps,)),
        ],
        compiler_params=roomy(20),
        name="update",
    )(spot, *held_in(pltpu.VMEM, *norms, *quarters), *held_in(pltpu.HBM, *stats))


def share_out(pieces, axis):
    return lax.all_to_all(pieces, axis, split_axis=0, concat_axis=0, tiled=True)


def swap(piece, distance):
    count = lax.axis_size("tile")
    return lax.ppermute(piece, "tile", [(i, i ^ distance) for i in range(count)])


def on_device(
    pixels,
    buckets,
    slot_owner_table,
    out_grad,
    master,
    left_stat,
    right_stat,
    left_root,
    right_root,
    vectors,
    moment,
):
    tile_count = lax.axis_size("tile")
    tile_place = lax.axis_index("tile")
    slot_count = pixels.shape[2]
    group_count = tile_count // STRIPS
    pairs = group_count // 2
    owned = master.shape[0]
    slots = owned * tile_count
    batch_count = lax.axis_size("batch")
    spot = lax.axis_index("batch").astype(jnp.int32).reshape(1)
    extra = extra_of(owned, batch_count)
    strips = share_out(pixels.reshape((tile_count,) + pixels.shape[3:]), "tile")
    dense = pack(master)
    paired = tile_count <= 8
    if paired:
        mine = [dense] + [swap(dense, 2 * k) for k in range(1, tile_count // 2)]
        pieces = mine + [swap(piece, 1) for piece in mine]
    else:
        pieces = [lax.all_gather(dense, "tile", axis=0, tiled=True)]

    numbers = jnp.arange(slots, dtype=jnp.int32)
    slot_of = jnp.sum(
        jnp.where(slot_owner_table[None, :] == numbers[:, None], numbers[None, :], 0), axis=1
    )
    owner = slot_of // owned
    within = slot_of - owner * owned
    place_of = slot_of
    if paired:
        apart = owner ^ tile_place
        apart = (apart & 1) * (tile_count // 2) + (apart >> 1)
        slot_of = place_of = within + owned * apart
    half = slots // 2
    near_place = jnp.where(place_of < half, place_of, half)
    far_place = jnp.where(place_of < half, half, place_of - half)
    image_ids = lax.dynamic_index_in_dim(
        buckets.reshape(group_count, slot_count), tile_place, 1, keepdims=False
    )
    turned = image_ids >= 2
    heights = jnp.where(image_ids == 0, 5 * CH // 9, jnp.where(image_ids == 1, 7 * CH // 9, CH))
    breadths = jnp.where(image_ids == 0, CW, jnp.where(image_ids == 1, 7 * CW // 9, 5 * CW // 9))
    sizes = jnp.stack(
        [
            jnp.where(turned, breadths, heights),
            jnp.where(turned, heights, breadths),
            turned,
        ],
        axis=1,
    )
    sizes = sizes.reshape(-1).astype(jnp.int32)

    two = 6 * C2 + HID2 + C2
    vec_two = jnp.concatenate([vectors[: 6 * C2], vectors[6 * C2 + HID2 : two]]).reshape(7, C2)
    vec_hid_two = vectors[6 * C2 : 6 * C2 + HID2].reshape(1, HID2)
    wide_end = two + 7 * C3
    vec_three = jnp.concatenate([vectors[two:wide_end], vectors[wide_end + HID3 :]])
    vec_three = jnp.pad(vec_three.reshape(8, C3), ((0, 0), (0, WIDE - C3)))
    vec_hid_three = vectors[wide_end : wide_end + HID3].reshape(1, HID3)

    flips = turned.reshape(-1, 1, 1, 1)
    goal = out_grad.reshape(2 * pairs, H3, W3, C3)
    goal = jnp.where(flips, goal.transpose(0, 2, 1, 3), goal)[:, :LINES]
    goal = goal.reshape(pairs, 2, LINES, W3, C3).transpose(0, 2, 3, 1, 4)
    goal = goal.reshape(pairs, LINES, 2 * W3, C3)
    goal = jnp.pad(goal, ((0, 0), (0, 0), (0, LINE - 2 * W3), (0, WIDE - C3)))
    goal = goal.reshape(pairs, AREA, WIDE)

    weights = run_unpack(slot_of, pieces)
    state = run_entry(sizes, strips, vec_two)
    result, *back, near, far, flat = run_main(
        (near_place, far_place),
        sizes,
        state,
        goal,
        (vec_two, vec_hid_two, vec_three, vec_hid_three),
        weights,
        tile_count,
    )
    pixel_back, vector = run_exit(sizes, state, back, flat, vec_two, tile_count)
    if paired:
        own, *parts = fold_pair(near, swap(far, 1), tile_count // 2)
        pieces = [own] + [swap(part, 2 * k + 2) for k, part in enumerate(parts)]
        vector, _ = lax.optimization_barrier((vector, parts[0]))
        vector = vector + swap(vector, 1)
        vectors_in = [vector] + [swap(vector, 2 * k) for k in range(1, tile_count // 2)]
    else:
        outgoing = jnp.concatenate([near[:half], far[:half]], axis=0)
        pieces = list(share_out(outgoing.reshape(tile_count, owned, HALF, 128), "tile"))
        vectors_in = list(lax.all_gather(vector, "tile"))
    result, pieces[1] = lax.optimization_barrier((result, pieces[1]))
    result = result.reshape(pairs, LINES, LINE, WIDE)[:, :, : 2 * W3, :C3]
    result = result.reshape(pairs, LINES, W3, 2, C3).transpose(0, 3, 1, 2, 4)
    result = result.reshape(2 * pairs, LINES, W3, C3)
    result = jnp.pad(result, ((0, 0), (0, H3 - LINES), (0, 0), (0, 0)))
    result = jnp.where(flips, result.transpose(0, 2, 1, 3), result)
    result = result.reshape(out_grad.shape)
    result = with_layout_constraint(result, Layout(major_to_minor=(0, 1, 2, 4, 5, 3, 6)))
    result, vectors_in[0] = lax.optimization_barrier((result, vectors_in[0]))
    own, *parts = fold_tile(spot, pieces, vectors_in, extra, batch_count)
    pixel_back, parts[0] = lax.optimization_barrier((pixel_back, parts[0]))
    returned = share_out(pixel_back, "tile")
    parts = [
        lax.ppermute(part, "batch", [(i, (i + k + 1) % batch_count) for i in range(batch_count)])
        for k, part in enumerate(parts)
    ]
    quarter = fold_batch(spot, [own] + parts, owned, tile_count)
    quarters = [quarter] + [
        lax.ppermute(quarter, "batch", [(i, (i + k) % batch_count) for i in range(batch_count)])
        for k in range(1, batch_count)
    ]
    returned = returned.astype(f32).reshape(pixels.shape)
    returned = with_layout_constraint(returned, Layout(major_to_minor=(0, 1, 3, 4, 2, 5)))
    returned, result, quarters[-1] = lax.optimization_barrier((returned, result, quarters[-1]))
    norm = square_sum(spot, quarters)
    if paired:
        norm = norm + swap(norm, 1)
        norms = [norm] + [swap(norm, 2 * k) for k in range(1, tile_count // 2)]
        norms += [jnp.zeros_like(norm)] * (4 - len(norms))
    else:
        norm = jnp.broadcast_to(norm[None], (tile_count,) + norm.shape)
        norms = [jnp.sum(share_out(norm, "tile"), axis=0)]
        norms += [jnp.zeros_like(norms[0])] * 3
    block_grad, left_new, right_new, master_new, weight_copy, whole_vector, clip = update(
        spot, norms, quarters, extra, master, left_stat, right_stat, left_root, right_root
    )
    clip_norm = clip[0, 0]
    share = vectors.shape[0] // tile_count
    whole_vector = whole_vector.reshape(-1)
    vec_grad = lax.dynamic_slice_in_dim(whole_vector, tile_place * share, share, 0)
    vec_moment = moment + vec_grad * vec_grad
    own_vectors = lax.dynamic_slice_in_dim(vectors, tile_place * share, share, 0)
    vec_new = own_vectors - rate_vector * vec_grad / (jnp.sqrt(vec_moment) + eps_adagrad)
    return (
        result,
        returned,
        clip_norm,
        block_grad,
        left_new,
        right_new,
        master_new,
        weight_copy,
        vec_grad,
        vec_moment,
        vec_new,
    )


def solution(mesh):
    placed = (
        P("batch", "tile", None, None, None, None),
        P("batch"),
        P(),
        P("batch", "tile", None, None, None, None, None),
        P("tile", None, None),
        P("tile", None, None),
        P("tile", None, None),
        P("tile", None, None),
        P("tile", None, None),
        P(),
        P("tile"),
    )
    return jax.shard_map(
        on_device,
        mesh=mesh,
        in_specs=placed,
        out_specs=(
            P("batch", "tile", None, None, None, None, None),
            P("batch", "tile", None, None, None, None),
            P(),
            P("tile", None, None),
            P("tile", None, None),
            P("tile", None, None),
            P("tile", None, None),
            P("tile", None, None),
            P("tile"),
            P("tile"),
            P("tile"),
        ),
        check_vma=False,
    )
```

```python
import functools

import jax
import jax.numpy as jnp
from jax import lax
from jax.experimental import pallas as pl
from jax.experimental.layout import Layout, with_layout_constraint
from jax.experimental.pallas import tpu as pltpu
from jax.sharding import PartitionSpec as P

C2 = 128
HID2 = 512
C3 = 320
HID3 = 1280
CH = 36
CW = 36
STRIPS = 4
BS = 64
SR = CH // STRIPS
H3 = CH // 2
W3 = CW // 2
LONG = 7 * CH // 9
LINES = LONG // 2
WIDE = 384
LINE = 40
AREA = LINES * LINE
STEP = 2 * LINE
STEPS = AREA // STEP
HALF = BS // 2

eps_norm = 1e-05
clip_limit = 1.0
rate_matrix = 0.3
rate_vector = 0.3
eps_adagrad = 1e-08
f32 = jnp.float32
bf16 = jnp.bfloat16

SHAPES = [(C2, HID2), (HID2, C2), (9 * C2, C3), (C3, HID3), (HID3, C3)]
USED = sum(rows // BS * (cols // BS) for rows, cols in SHAPES)
VEC_ROWS = (6 * C2 + HID2 + C2 + C3 + 6 * C3 + HID3 + C3) // 128


VEC_BLOCKS = -(-VEC_ROWS // HALF)


def extra_of(owned, groups):
    return VEC_BLOCKS + -(owned + VEC_BLOCKS) % groups


def product(left, right):
    return jnp.dot(left, right, preferred_element_type=f32)


def product_nt(left, right):
    return lax.dot_general(left, right, (((1,), (1,)), ((), ())), preferred_element_type=f32)


def product_tn(left, right):
    return lax.dot_general(left, right, (((0,), (0,)), ((), ())), preferred_element_type=f32)


def gelu_pair(values):
    bell = jnp.exp2(values * values * (-0.5 * 1.4426950408889634))
    step = pl.reciprocal(1.0 + (0.3275911 * 0.7071067811865476) * jnp.abs(values), approx=True)
    tail = step * (
        0.5 * 0.254829592
        + step
        * (
            0.5 * -0.284496736
            + step
            * (0.5 * 1.421413741 + step * (0.5 * -1.453152027 + step * (0.5 * 1.061405429)))
        )
    )
    tail = tail * bell
    share = jnp.where(values >= 0.0, 1.0 - tail, tail)
    return (values * share, share + values * (bell * 0.3989422804014327))


def fold(values):
    chans = values.shape[-1]
    return jnp.sum(values.reshape(-1, 8, chans), axis=0)


def by_image(total):
    total = total + pltpu.roll(total, 4, 0)
    total = total + pltpu.roll(total, 2, 0)
    return jnp.sum(total, axis=1, keepdims=True)


def line(pattern):
    return jnp.concatenate([pattern] * (LINE // 8), axis=0)


def spread(pattern, chans):
    return jnp.broadcast_to(pattern, (8, chans))


def affine(values, factor, shift):
    tiles = values.reshape(-1, 8, values.shape[-1])
    return (tiles * factor + shift).reshape(values.shape)


def scaled(values, factor):
    tiles = values.reshape(-1, 8, values.shape[-1])
    return (tiles * factor).reshape(values.shape)


def from_left(values):
    return pltpu.roll(values, 2, 0)


def from_right(values):
    return pltpu.roll(values, values.shape[0] - 2, 0)


def rounded(values):
    return values.astype(bf16).astype(f32)


def widen(values):
    return jnp.concatenate([values] * (WIDE // 128), axis=-1)


def norm_terms(total, square, count):
    mean = by_image(total) / count
    scaling = lax.rsqrt(by_image(square) / count - mean * mean + eps_norm)
    return (mean, scaling)


def sweep(visit, start):
    return lax.fori_loop(0, STEPS, visit, start, unroll=True)


def step_rows(k, lines=0):
    start = k * STEP + lines * LINE
    return pl.ds(start if isinstance(k, int) else pl.multiple_of(start, LINE), STEP)


def held_in(space, *arrays):
    return [pltpu.with_memory_space_constraint(array, space) for array in arrays]


VMEM_BLOCK = pl.BlockSpec(memory_space=pltpu.VMEM)
HBM = pl.BlockSpec(memory_space=pltpu.HBM)
SMEM = pl.BlockSpec(memory_space=pltpu.SMEM)


def roomy(mebibytes):
    return pltpu.CompilerParams(vmem_limit_bytes=mebibytes * 1024 * 1024)


class Geometry:
    def __init__(self, size_ref, pair):
        parity = lax.broadcasted_iota(jnp.int32, (8, 128), 0) % 2
        high, broad, turned = (
            jnp.where(parity == 0, size_ref[pair * 6 + n], size_ref[pair * 6 + 3 + n])
            for n in range(3)
        )
        self.high = high
        self.count_two = (high * broad * C2).astype(f32)[:, :1]
        self.high3 = (high + 1) // 2
        broad3 = (broad + 1) // 2
        self.count_three = (self.high3 * broad3 * C3).astype(f32)[:, :1]
        place = lax.broadcasted_iota(jnp.int32, (LINE, 128), 0) // 2
        inside = lax.broadcasted_iota(jnp.int32, (LINE, 128), 0) < 2 * W3
        self.reach = []
        self.col_share = []
        for pc in range(2):
            column = 2 * place + pc
            self.reach.append(jnp.where(inside & (column < line(broad)), line(high), 0))
            edge = (column == 0) | (column == line(broad) - 1)
            self.col_share.append(jnp.where(edge, 0.5, 1.0 / 3.0))
        self.reach3 = jnp.where(inside & (place < line(broad3)), line(self.high3), 0)
        edge3 = (place == 0) | (place == line(broad3) - 1)
        self.col_share3 = jnp.where(edge3, 0.5, 1.0 / 3.0)
        self.flipped = jnp.concatenate([turned] * (STEP // 8), axis=0) > 0

    def share(self, plane, k):
        pr, pc = plane // 2, plane % 2
        return self.lines(4 * k + pr, 2, self.reach[pc], self.col_share[pc], self.high)

    def share3(self, k):
        return self.lines(2 * k, 1, self.reach3, self.col_share3, self.high3)

    def lines(self, row, stride, reach, col_share, height):
        parts = []
        for n in range(2):
            here = row + stride * n
            row_share = jnp.where((here == 0) | (here == height - 1), 0.5, 1.0 / 3.0)
            parts.append(jnp.where(here < reach, line(row_share) * col_share, 0.0))
        return jnp.concatenate(parts, axis=0)


def strip_place(pair, spot, strip_count):
    return lax.rem(pair * 8 + strip_count - 2 + spot, strip_count)


def each_image(size_ref, pair, visit):
    for image in range(2):
        way = size_ref[pair * 6 + 3 * image + 2]
        for flat in (True, False):

            @pl.when(way == (0 if flat else 1))
            def _():
                def one(r, carry):
                    for pr in range(2):
                        for pc in range(2):
                            line_place = pl.ds(r * LINE + image, W3, stride=2)
                            if flat:
                                there = pl.ds((2 * r + pr) * LINE + pc, W3, stride=2)
                            else:
                                there = pl.ds(pc * LINE + 2 * r + pr, W3, stride=2 * LINE)
                            visit(image, pr * 2 + pc, line_place, there)
                    return carry

                lax.fori_loop(0, LINES, one, 0)


def row_windows(col_ref, pc, k):
    both = col_ref[pc, step_rows(k, 1)] + col_ref[2 + pc, step_rows(k, 1)]
    return (both + col_ref[2 + pc, step_rows(k)], both + col_ref[pc, step_rows(k, 2)])


def put_col_windows(col_ref, pr, k, even, odd):
    both = even + odd
    col_ref[pr * 2, step_rows(k, 1)] = both + from_left(odd)
    col_ref[pr * 2 + 1, step_rows(k, 1)] = both + from_right(even)


def clear_edges(col_ref):
    zero_line = jnp.zeros((LINE, C2), f32)
    for plane in range(4):
        col_ref[plane, 0:LINE] = zero_line
        col_ref[plane, AREA + LINE : AREA + 2 * LINE] = zero_line


def entry_kernel(
    pairs,
    strip_count,
    size_ref,
    strips_ref,
    vec_two_ref,
    x_out,
    inv_out,
    pool_out,
    mix_out,
    stat_out,
    image_ref,
    col_ref,
):
    pair = pl.program_id(0) if pairs > 1 else 0
    x_ref, inv_ref, pool_ref, mix_ref = (ref.at[0] for ref in (x_out, inv_out, pool_out, mix_out))
    shape = Geometry(size_ref, pair)
    gain1, bias1, scale1 = (vec_two_ref[n : n + 1] for n in range(3))
    clear_edges(col_ref)

    def to_rows(within, carry):
        for spot in range(2 * STRIPS):
            image, strip = spot // STRIPS, spot % STRIPS
            start = pl.multiple_of((strip * SR + within) * LINE, LINE)
            source = strip_place(pair, spot, strip_count)
            image_ref[image, pl.ds(start, CW)] = strips_ref[source, within].astype(f32)
        return carry

    lax.fori_loop(0, SR, to_rows, 0)

    def take_in(image, plane, line_place, there):
        x_ref[plane, line_place] = image_ref[image, there]

    each_image(size_ref, pair, take_in)

    def arrange(k, carry):
        total, square = carry
        rows = step_rows(k)
        for plane in range(4):
            share = shape.share(plane, k)
            inv_ref[plane, rows] = share
            values = jnp.where(share > 0.0, x_ref[plane, rows], 0.0)
            x_ref[plane, rows] = values
            total = total + fold(values)
            square = square + fold(values * values)
        return (total, square)

    nothing = jnp.zeros((8, C2), f32)
    total, square = sweep(arrange, (nothing, nothing))
    mean1, scaling1 = norm_terms(total, square, shape.count_two)
    factor1 = scaling1 * gain1
    shift1 = bias1 - mean1 * scaling1 * gain1

    def window_cols(k, carry):
        rows = step_rows(k)
        for pr in range(2):
            masked = []
            for pc in range(2):
                plane = pr * 2 + pc
                normal = rounded(affine(x_ref[plane, rows], factor1, shift1))
                masked.append(jnp.where(inv_ref[plane, rows] > 0.0, normal, 0.0))
            put_col_windows(col_ref, pr, k, *masked)
        return carry

    sweep(window_cols, 0)

    def mix(k, carry):
        total, square = carry
        rows = step_rows(k)
        for pc in range(2):
            windows = row_windows(col_ref, pc, k)
            for pr in range(2):
                plane = pr * 2 + pc
                values = x_ref[plane, rows]
                share = inv_ref[plane, rows]
                pooled = windows[pr] * share - rounded(affine(values, factor1, shift1))
                pooled = jnp.where(share > 0.0, pooled, 0.0)
                mixed = values + scale1 * pooled
                pool_ref[plane, rows] = pooled
                mix_ref[plane, rows] = mixed
                total = total + fold(mixed)
                square = square + fold(mixed * mixed)
        return (total, square)

    total, square = sweep(mix, (nothing, nothing))
    mean2, scaling2 = norm_terms(total, square, shape.count_two)
    for n, value in enumerate((mean1, scaling1, mean2, scaling2)):
        stat_out[0, n] = spread(value, 128)


def pair_specs(pairs, shapes, mode=None):
    if pairs == 1:
        return [VMEM_BLOCK] * len(shapes)
    return [
        pl.BlockSpec(
            (1,) + shape, lambda t, rank=len(shape): (t,) + (0,) * rank, pipeline_mode=mode
        )
        for shape in shapes
    ]


def whole_specs(pairs, shapes):
    if pairs == 1:
        return [VMEM_BLOCK] * len(shapes)
    return [
        pl.BlockSpec(
            shape,
            lambda t, rank=len(shape): (0,) * rank,
            pipeline_mode=pl.Buffered(1),
        )
        for shape in shapes
    ]


def pair_arrays(pairs, shapes, kinds):
    make = pltpu.VMEM if pairs == 1 else jax.ShapeDtypeStruct
    return [make((pairs,) + shape, kind) for shape, kind in zip(shapes, kinds)]


STATE = [(4, AREA, C2)] * 4 + [(4, 8, 128)]
BACK = [(4, AREA, C2)] * 2 + [(2, 8, 128)]


def run_entry(sizes, strips, vec_two):
    strip_count = strips.shape[0]
    pairs = strip_count // 8
    return pl.pallas_call(
        functools.partial(entry_kernel, pairs, strip_count),
        grid=() if pairs == 1 else (pairs,),
        in_specs=[SMEM] + whole_specs(pairs, [strips.shape, vec_two.shape]),
        out_specs=pair_specs(pairs, STATE),
        out_shape=pair_arrays(pairs, STATE, [f32] * 5),
        scratch_shapes=[
            pltpu.VMEM((2, CH * LINE, C2), f32),
            pltpu.VMEM((4, AREA + 2 * LINE, C2), f32),
        ],
        compiler_params=roomy(6 if pairs == 1 else 40),
        name="entry",
    )(sizes, strips, vec_two)


WEIGHTS = [(C2, HID2), (HID2, C2), (9 * C2, WIDE), (WIDE, HID3), (HID3, WIDE)]


def unpack_kernel(piece_count, slot_ref, *refs):
    piece_refs, refs = refs[:piece_count], refs[piece_count:]
    weights, gathered_ref = refs[:-1], refs[-1]
    count = piece_refs[0].shape[0]
    for n, ref in enumerate(piece_refs):
        gathered_ref[n * count : n * count + count] = ref[...]
    left_half = lax.broadcasted_iota(jnp.int32, (HALF, 128), 1) < BS
    offset = 0
    for (rows, cols), ref in zip(SHAPES, weights):
        wide = cols // BS
        for rb in range(rows // BS):
            for cb in range(0, wide, 2):
                number = offset + rb * wide + cb
                first = gathered_ref[slot_ref[number]]
                turned = pltpu.roll(first, BS, 1)
                if cb + 1 < wide:
                    second = gathered_ref[slot_ref[number + 1]]
                    top = jnp.where(left_half, first, pltpu.roll(second, BS, 1))
                    low = jnp.where(left_half, turned, second)
                else:
                    top = jnp.where(left_half, first, 0.0)
                    low = jnp.where(left_half, turned, 0.0)
                place = slice(cb * BS, cb * BS + 128)
                ref[rb * BS : rb * BS + HALF, place] = top
                ref[rb * BS + HALF : rb * BS + BS, place] = low
        offset += rows // BS * wide
    weights[3][C3:, :] = jnp.zeros((WIDE - C3, HID3), bf16)


def run_unpack(slot_of, pieces):
    slots = sum(piece.shape[0] for piece in pieces)
    return pl.pallas_call(
        functools.partial(unpack_kernel, len(pieces)),
        in_specs=[SMEM] + [VMEM_BLOCK] * len(pieces),
        out_specs=[VMEM_BLOCK] * 5,
        out_shape=[pltpu.VMEM(shape, bf16) for shape in WEIGHTS],
        scratch_shapes=[pltpu.VMEM((slots, HALF, 128), bf16)],
        compiler_params=roomy(6),
        name="unpack",
    )(slot_of, *held_in(pltpu.VMEM, *pieces))


def main_kernel(
    pairs,
    strip_count,
    slots,
    near_place,
    far_place,
    size_ref,
    inv_in,
    mix_in,
    stat_in,
    goal_ref,
    vec_two_ref,
    vec_hid_two_ref,
    vec_three_ref,
    vec_hid_three_ref,
    w1_ref,
    w2_ref,
    we_ref,
    w3_ref,
    w4_ref,
    result_ref,
    zed_out,
    dx_out,
    mean_out,
    near_ref,
    far_ref,
    flat_ref,
    zed_ref,
    hid_ref,
    u_ref,
    g_ref,
    h_ref,
    dy_ref,
    patch_ref,
    dpatch_ref,
    inv3_ref,
    e_ref,
    col3_ref,
    pool3_ref,
    mix3_ref,
    dx3_ref,
    hid3_ref,
    dhid3_ref,
    u3_ref,
    g3_ref,
    h3_ref,
    dy3_ref,
    dpre_ref,
    gw1_ref,
    gw2_ref,
    gwe_ref,
    gw3_ref,
    gw4_ref,
    acc_two,
    acc_hid_two,
    acc_three,
    acc_hid_three,
):
    pair = pl.program_id(0) if pairs > 1 else 0
    grads = [gw1_ref, gw2_ref, gwe_ref, gw3_ref, gw4_ref]
    inv_ref, mix_ref, stat_ref = (ref.at[0] for ref in (inv_in, mix_in, stat_in))
    back_ref, dx_ref = zed_out.at[0], dx_out.at[0]
    left_half = lax.broadcasted_iota(jnp.int32, (HALF, 128), 1) < BS

    def at_pair(number, act):
        if pairs == 1:
            act()
        else:
            pl.when(pair == number)(act)

    def begin():
        acc_two[...] = jnp.zeros(acc_two.shape, f32)
        acc_hid_two[...] = jnp.zeros(acc_hid_two.shape, f32)
        acc_three[...] = jnp.zeros(acc_three.shape, f32)
        acc_hid_three[...] = jnp.zeros(acc_hid_three.shape, f32)

    at_pair(0, begin)
    shape = Geometry(size_ref, pair)
    count_two, count_three, flipped = shape.count_two, shape.count_three, shape.flipped
    nothing = jnp.zeros((8, C2), f32)
    nothing3 = jnp.zeros((8, WIDE), f32)
    gain2, bias2, scale2, out_bias = (vec_two_ref[n : n + 1] for n in range(3, 7))
    embed_bias, gain3, bias3, scale3 = (vec_three_ref[n : n + 1] for n in range(4))
    gain4, bias4, scale4, out_bias3 = (vec_three_ref[n : n + 1] for n in range(4, 8))
    mean2, scaling2 = stat_ref[2], stat_ref[3]
    factor2 = scaling2 * gain2
    shift2 = bias2 - mean2 * scaling2 * gain2
    for plane in range(4):
        zed_ref[plane, 0:LINE] = jnp.zeros((LINE, C2), f32)
    col3_ref[0:LINE] = jnp.zeros((LINE, WIDE), f32)
    col3_ref[AREA + LINE : AREA + 2 * LINE] = jnp.zeros((LINE, WIDE), f32)

    def put_block(number, block):
        near_ref[near_place[number]] = block
        far_ref[far_place[number]] = block

    def pack_blocks(matrices):
        offsets = [0]
        for rows, cols in SHAPES:
            offsets.append(offsets[-1] + rows // BS * (cols // BS))
        for which in matrices:
            (rows, cols), ref = SHAPES[which], grads[which]
            wide = cols // BS
            for rb in range(rows // BS):
                for cb in range(0, wide, 2):
                    number = offsets[which] + rb * wide + cb
                    at = slice(cb * BS, cb * BS + 128)
                    top = ref[rb * BS : rb * BS + HALF, at].astype(bf16)
                    low = ref[rb * BS + HALF : rb * BS + BS, at].astype(bf16)
                    put_block(number, jnp.where(left_half, top, pltpu.roll(low, BS, 1)))
                    if cb + 1 < wide:
                        put_block(number + 1, jnp.where(left_half, pltpu.roll(top, BS, 1), low))

    def plane_rows(plane):
        return slice(plane * AREA, plane * AREA + AREA)

    def begin_plane(plane):
        low = affine(mix_ref[plane], factor2, shift2).astype(bf16)
        h_ref[plane_rows(plane)] = low
        hid_ref[plane % 2] = product(low, w1_ref[...])

    begin_plane(0)
    for plane in range(4):
        if plane < 3:
            begin_plane(plane + 1)
        for k in range(STEPS):
            rows = step_rows(k)
            flat = slice(plane * AREA + k * STEP, plane * AREA + k * STEP + STEP)
            for at in range(0, HID2, 128):
                lanes = slice(at, at + 128)
                active, slope = gelu_pair(hid_ref[plane % 2, rows, lanes] + vec_hid_two_ref[:, lanes])
                u_ref[flat, lanes] = active.astype(bf16)
                g_ref[flat, lanes] = slope.astype(bf16)
        out = product(u_ref[plane_rows(plane)], w2_ref[...]) + out_bias
        zed = jnp.where(inv_ref[plane] > 0.0, mix_ref[plane] + scale2 * out, 0.0)
        zed_ref[plane, LINE : LINE + AREA] = rounded(zed)

    def patches(k, carry):
        rows = step_rows(k)
        taps = []
        for ky in range(3):
            pr = (0 if ky == 1 else 1) * 2
            source = step_rows(k, 0 if ky == 0 else 1)
            even = zed_ref[pr, source]
            odd = zed_ref[pr + 1, source]
            taps.append((from_left(odd), even, odd))
        for ky in range(3):
            for kx in range(3):
                at = (3 * ky + kx) * C2
                tap = taps[ky][kx]
                if ky != kx:
                    tap = jnp.where(flipped, taps[kx][ky], tap)
                patch_ref[rows, at : at + C2] = tap.astype(bf16)
        return carry

    sweep(patches, 0)
    e_ref[...] = product(patch_ref[...], we_ref[...])

    def embed(k, carry):
        total, square = carry
        rows = step_rows(k)
        share = shape.share3(k)
        inv3_ref[rows] = share
        out = jnp.where(widen(share) > 0.0, e_ref[rows] + embed_bias, 0.0)
        e_ref[rows] = out
        return (total + fold(out), square + fold(out * out))

    total, square = sweep(embed, (nothing3, nothing3))
    mean3, scaling3 = norm_terms(total, square, count_three)
    factor3 = scaling3 * gain3
    shift3 = bias3 - mean3 * scaling3 * gain3

    def window_cols3(k, carry):
        rows = step_rows(k)
        normal = rounded(affine(e_ref[rows], factor3, shift3))
        masked = jnp.where(widen(inv3_ref[rows]) > 0.0, normal, 0.0)
        col3_ref[step_rows(k, 1)] = masked + from_left(masked) + from_right(masked)
        return carry

    sweep(window_cols3, 0)

    def row_windows3(k):
        return col3_ref[step_rows(k)] + col3_ref[step_rows(k, 1)] + col3_ref[step_rows(k, 2)]

    def mix3(k, carry):
        total, square = carry
        rows = step_rows(k)
        values = e_ref[rows]
        share = widen(inv3_ref[rows])
        pooled = row_windows3(k) * share - rounded(affine(values, factor3, shift3))
        pooled = jnp.where(share > 0.0, pooled, 0.0)
        mixed = values + scale3 * pooled
        pool3_ref[rows] = pooled
        mix3_ref[rows] = mixed
        return (total + fold(mixed), square + fold(mixed * mixed))

    total, square = sweep(mix3, (nothing3, nothing3))
    mean4, scaling4 = norm_terms(total, square, count_three)
    factor4 = scaling4 * gain4
    shift4 = bias4 - mean4 * scaling4 * gain4
    normal4 = (spread(scaling4, WIDE), spread(-mean4 * scaling4, WIDE))

    def prepare3(k, d_bias):
        rows = step_rows(k)
        h3_ref[rows] = affine(mix3_ref[rows], factor4, shift4).astype(bf16)
        goal = goal_ref[0, rows].astype(f32)
        goal = jnp.where(widen(inv3_ref[rows]) > 0.0, goal, 0.0)
        low_goal = (scale4 * goal).astype(bf16)
        dy3_ref[rows] = low_goal
        return d_bias + fold(low_goal.astype(f32))

    acc_three[7] += sweep(prepare3, nothing3)

    def keep(ref, value, place=slice(None)):
        if pairs == 1:
            ref[place] = value.astype(ref.dtype)
        else:

            @pl.when(pair == 0)
            def _():
                ref[place] = value

            @pl.when(pair > 0)
            def _():
                ref[place] += value

    def begin_chunk(at):
        lanes = slice(at, at + 256)
        hid3_ref[:, lanes] = product(h3_ref[...], w3_ref[:, lanes])
        dhid3_ref[:, lanes] = product_nt(dy3_ref[...], w4_ref[lanes])

    begin_chunk(0)
    for at in range(0, HID3, 256):
        if at + 256 < HID3:
            begin_chunk(at + 256)
        for lane in (at, at + 128):
            lanes = slice(lane, lane + 128)
            total = nothing
            for k in range(STEPS):
                rows = step_rows(k)
                active, slope = gelu_pair(hid3_ref[rows, lanes] + vec_hid_three_ref[:, lanes])
                u3_ref[rows, lanes] = active.astype(bf16)
                low = (slope * dhid3_ref[rows, lanes]).astype(bf16)
                g3_ref[rows, lanes] = low
                total = total + fold(low.astype(f32))
            acc_hid_three[:, lanes] += total
        lanes = slice(at, at + 256)
        out = product(u3_ref[:, lanes], w4_ref[lanes])
        d_low = product_nt(g3_ref[:, lanes], w3_ref[:, lanes])
        result_ref[0] = out if at == 0 else result_ref[0] + out
        dx3_ref[...] = d_low if at == 0 else dx3_ref[...] + d_low
        keep(gw3_ref, product_tn(h3_ref[...], g3_ref[:, lanes]), (slice(None), lanes))
        keep(gw4_ref, product_tn(u3_ref[:, lanes], dy3_ref[...]), lanes)

    def finish3(k, carry):
        d_scale, d_shift, d_gain = carry
        rows = step_rows(k)
        valid = widen(inv3_ref[rows]) > 0.0
        mixed = mix3_ref[rows]
        out = jnp.where(valid, result_ref[0, rows] + out_bias3, 0.0)
        result_ref[0, rows] = mixed + scale4 * out
        d_scale = d_scale + fold(out * goal_ref[0, rows].astype(f32))
        d_low = dx3_ref[rows]
        normal = affine(mixed, *normal4)
        return (d_scale, d_shift + fold(d_low), d_gain + fold(d_low * normal))

    d_scale, d_shift, d_gain = sweep(finish3, (nothing3, nothing3, nothing3))
    acc_three[6] += d_scale
    acc_three[5] += d_shift
    acc_three[4] += d_gain
    mean_shift = by_image(d_shift * gain4) / count_three
    mean_gain = by_image(d_gain * gain4) / count_three
    back_gain4 = scaling4 * gain4
    back_mean4 = spread(-scaling4 * mean_shift, WIDE)
    back_normal4 = spread(scaling4 * mean_gain, WIDE)

    def unmix3(k, d_scale):
        rows = step_rows(k)
        share = widen(inv3_ref[rows])
        valid = share > 0.0
        normal = affine(mix3_ref[rows], *normal4)
        back = affine(dx3_ref[rows], back_gain4, back_mean4) - scaled(normal, back_normal4)
        d_mixed = jnp.where(valid, back + goal_ref[0, rows].astype(f32), 0.0)
        dx3_ref[rows] = d_mixed
        d_scale = d_scale + fold(pool3_ref[rows] * d_mixed)
        weighted = scale3 * d_mixed * share
        col3_ref[step_rows(k, 1)] = weighted + from_left(weighted) + from_right(weighted)
        return d_scale

    acc_three[3] += sweep(unmix3, nothing3)
    normal3 = (spread(scaling3, WIDE), spread(-mean3 * scaling3, WIDE))

    def unpool3(k, carry):
        d_shift, d_gain = carry
        rows = step_rows(k)
        valid = widen(inv3_ref[rows]) > 0.0
        d_normal = jnp.where(valid, row_windows3(k) - scale3 * dx3_ref[rows], 0.0)
        pool3_ref[rows] = d_normal
        normal = affine(e_ref[rows], *normal3)
        return (d_shift + fold(d_normal), d_gain + fold(d_normal * normal))

    d_shift, d_gain = sweep(unpool3, (nothing3, nothing3))
    acc_three[2] += d_shift
    acc_three[1] += d_gain
    mean_shift = by_image(d_shift * gain3) / count_three
    mean_gain = by_image(d_gain * gain3) / count_three
    back_gain3 = scaling3 * gain3
    back_mean3 = spread(-scaling3 * mean_shift, WIDE)
    back_normal3 = spread(scaling3 * mean_gain, WIDE)

    def unnorm3(k, d_bias):
        rows = step_rows(k)
        valid = widen(inv3_ref[rows]) > 0.0
        normal = affine(e_ref[rows], *normal3)
        back = affine(pool3_ref[rows], back_gain3, back_mean3) - scaled(normal, back_normal3)
        low = jnp.where(valid, dx3_ref[rows] + back, 0.0).astype(bf16)
        dpre_ref[rows] = low
        return d_bias + fold(low.astype(f32))

    acc_three[0] += sweep(unnorm3, nothing3)
    keep(gwe_ref, product_tn(patch_ref[...], dpre_ref[...]))
    dpatch_ref[0:AREA] = product_nt(dpre_ref[...], we_ref[...])
    dpatch_ref[AREA : AREA + LINE] = jnp.zeros((LINE, 9 * C2), f32)

    def gather_back(k, carry):
        rows = step_rows(k)

        def tap(ky, kx, source):
            at = (3 * ky + kx) * C2
            value = dpatch_ref[source, at : at + C2]
            if ky != kx:
                at = (3 * kx + ky) * C2
                value = jnp.where(flipped, dpatch_ref[source, at : at + C2], value)
            return value

        sources = []
        for ky in range(3):
            source = step_rows(k, 1 if ky == 0 else 0)
            sources.append(
                (tap(ky, 1, source), tap(ky, 2, source) + from_right(tap(ky, 0, source)))
            )
        for pc in range(2):
            for pr, value in ((0, sources[1][pc]), (1, sources[2][pc] + sources[0][pc])):
                plane = pr * 2 + pc
                valid = inv_ref[plane, rows] > 0.0
                back_ref[plane, rows] = jnp.where(valid, rounded(value), 0.0)
        return carry

    sweep(gather_back, 0)

    if pairs == 1:
        pack_blocks(range(2, 5))

    normal2 = (spread(scaling2, C2), spread(-mean2 * scaling2, C2))

    def begin_back(plane):
        low_goal = (scale2 * back_ref[plane]).astype(bf16)
        dy_ref[plane_rows(plane)] = low_goal
        hid_ref[plane % 2] = product_nt(low_goal, w2_ref[...])
        return fold(low_goal.astype(f32))

    d_out_bias = begin_back(0)
    d_shift, d_gain = nothing, nothing
    sums = [nothing] * (HID2 // 128)
    new_gw1, new_gw2 = None, None
    for plane in range(4):
        if plane < 3:
            d_out_bias = d_out_bias + begin_back(plane + 1)
        for k in range(STEPS):
            rows = step_rows(k)
            part = slice(plane * AREA + k * STEP, plane * AREA + k * STEP + STEP)
            for n, at in enumerate(range(0, HID2, 128)):
                lanes = slice(at, at + 128)
                low = g_ref[part, lanes].astype(f32) * hid_ref[plane % 2, rows, lanes]
                low = low.astype(bf16)
                g_ref[part, lanes] = low
                sums[n] = sums[n] + fold(low.astype(f32))
        flat = plane_rows(plane)
        d_low = product_nt(g_ref[flat], w1_ref[...])
        dx_ref[plane] = d_low
        d_shift = d_shift + fold(d_low)
        d_gain = d_gain + fold(d_low * affine(mix_ref[plane], *normal2))
        part_gw1 = product_tn(h_ref[flat], g_ref[flat])
        part_gw2 = product_tn(dy_ref[flat], u_ref[flat])
        new_gw1 = part_gw1 if plane == 0 else new_gw1 + part_gw1
        new_gw2 = part_gw2 if plane == 0 else new_gw2 + part_gw2
    new_gw2 = new_gw2.T
    for n, value in enumerate(sums):
        acc_hid_two[:, n * 128 : n * 128 + 128] += value
    acc_two[6] += d_out_bias
    acc_two[4] += d_shift
    acc_two[3] += d_gain
    mean_out[0, 0] = spread(by_image(d_shift * gain2) / count_two, 128)
    mean_out[0, 1] = spread(by_image(d_gain * gain2) / count_two, 128)
    keep(gw1_ref, new_gw1)
    keep(gw2_ref, new_gw2)
    d_scale = fold(w2_ref[...].astype(f32) * new_gw2) + out_bias * d_out_bias
    acc_two[5] += d_scale / scale2

    def finish():
        if pairs > 1:
            pack_blocks(range(5))
        else:
            pack_blocks(range(2))

        def filler(number, carry):
            put_block(number, jnp.zeros((HALF, 128), bf16))
            return carry

        lax.fori_loop(USED, slots, filler, 0)

        flat_ref[...] = jnp.zeros(flat_ref.shape, f32)

        def put(at, total, length):
            if at % 128:
                room = jnp.zeros((8, 128), f32)
                if total.shape[1] < length + BS:
                    total = jnp.concatenate([total, room], axis=1)
                total = pltpu.roll(total, BS, 1)
            whole = jnp.sum(total, axis=0, keepdims=True)
            done = -(at % 128)
            row = at // 128
            lane = 0
            while done < length:
                first = max(0, -done)
                last = min(128, length - done)
                flat_ref[row : row + 1, first:last] = whole[:, lane + first : lane + last]
                done += 128
                lane += 128
                row += 1

        at = 3 * C2
        for n in range(3, 6):
            put(at, acc_two[n], C2)
            at += C2
        put(at, acc_hid_two[...], HID2)
        at += HID2
        put(at, acc_two[6], C2)
        at += C2
        for n in range(7):
            put(at, acc_three[n], C3)
            at += C3
        put(at, acc_hid_three[...], HID3)
        at += HID3
        put(at, acc_three[7], C3)

    at_pair(pairs - 1, finish)


def run_main(places, sizes, state, goal, vectors, weights, strip_count):
    pairs = goal.shape[0]
    slots = places[0].shape[0]
    half = slots // 2 + 1
    if pairs == 1:
        state = held_in(pltpu.VMEM, *state)
    weights = held_in(pltpu.VMEM, *weights)
    _, inv, _, mix, stat = state
    state_shapes = [STATE[1], STATE[3], STATE[4]]
    grad_kind = bf16 if pairs == 1 else f32
    wide_f32 = pltpu.VMEM((AREA, WIDE), f32)
    wide_bf16 = pltpu.VMEM((AREA, WIDE), bf16)
    scratch = [
        pltpu.VMEM((4, AREA + LINE, C2), f32),
        pltpu.VMEM((2, AREA, HID2), f32),
        pltpu.VMEM((4 * AREA, HID2), bf16),
        pltpu.VMEM((4 * AREA, HID2), bf16),
        pltpu.VMEM((4 * AREA, C2), bf16),
        pltpu.VMEM((4 * AREA, C2), bf16),
        pltpu.VMEM((AREA, 9 * C2), bf16),
        pltpu.VMEM((AREA + LINE, 9 * C2), f32),
        pltpu.VMEM((AREA, 128), f32),
        wide_f32,
        pltpu.VMEM((AREA + 2 * LINE, WIDE), f32),
        wide_f32,
        wide_f32,
        wide_f32,
        pltpu.VMEM((AREA, HID3), f32),
        pltpu.VMEM((AREA, HID3), f32),
        pltpu.VMEM((AREA, HID3), bf16),
        pltpu.VMEM((AREA, HID3), bf16),
        wide_bf16,
        wide_bf16,
        wide_bf16,
        pltpu.VMEM((C2, HID2), grad_kind),
        pltpu.VMEM((HID2, C2), grad_kind),
        pltpu.VMEM((9 * C2, WIDE), grad_kind),
        pltpu.VMEM((WIDE, HID3), grad_kind),
        pltpu.VMEM((HID3, WIDE), grad_kind),
        pltpu.VMEM((7, 8, C2), f32),
        pltpu.VMEM((8, HID2), f32),
        pltpu.VMEM((8, 8, WIDE), f32),
        pltpu.VMEM((8, HID3), f32),
    ]
    out_shapes = [(half, HALF, 128), (half, HALF, 128), (VEC_BLOCKS * HALF, 128)]
    make = pltpu.VMEM if pairs == 1 else jax.ShapeDtypeStruct
    return pl.pallas_call(
        functools.partial(main_kernel, pairs, strip_count, slots),
        grid=() if pairs == 1 else (pairs,),
        in_specs=[SMEM] * 3
        + pair_specs(pairs, state_shapes + [goal.shape[1:]], pl.Buffered(1))
        + whole_specs(pairs, [vector.shape for vector in vectors])
        + [VMEM_BLOCK] * 5,
        out_specs=pair_specs(pairs, [(AREA, WIDE)] + BACK) + whole_specs(pairs, out_shapes),
        out_shape=pair_arrays(pairs, [(AREA, WIDE)] + BACK, [f32] * 4)
        + [make(shape, kind) for shape, kind in zip(out_shapes, (bf16, bf16, f32))],
        scratch_shapes=scratch,
        compiler_params=pltpu.CompilerParams(
            vmem_limit_bytes=(40 if pairs == 1 else 56) * 1024 * 1024,
            fuse_transposed_lhs_in_matmul=True,
        ),
        name="blocks",
    )(*places, sizes, inv, mix, stat, goal, *vectors, *weights)


def exit_kernel(
    pairs,
    strip_count,
    size_ref,
    x_in,
    inv_in,
    pool_in,
    mix_in,
    stat_in,
    zed_in,
    dx_in,
    mean_in,
    flat_ref,
    vec_two_ref,
    payload_hbm,
    vector_ref,
    payload_ref,
    image_ref,
    col_ref,
    dx_ref,
    back_ref,
    acc_ref,
    sem,
):
    pair = pl.program_id(0) if pairs > 1 else 0
    x_ref, inv_ref, pool_ref, mix_ref, stat_ref, zed_ref, low_ref, mean_ref = (
        ref.at[0] for ref in (x_in, inv_in, pool_in, mix_in, stat_in, zed_in, dx_in, mean_in)
    )
    shape = Geometry(size_ref, pair)
    count_two = shape.count_two
    gain1, bias1, scale1, gain2 = (vec_two_ref[n : n + 1] for n in range(4))
    mean1, scaling1, mean2, scaling2 = (stat_ref[n] for n in range(4))
    normal2 = (scaling2, -mean2 * scaling2)
    clear_edges(col_ref)
    nothing = jnp.zeros((8, C2), f32)
    back_gain2 = scaling2 * gain2
    back_mean2 = -scaling2 * mean_ref[0]
    back_normal2 = scaling2 * mean_ref[1]

    if pairs > 1:

        @pl.when(pair == 0)
        def _():
            acc_ref[...] = jnp.zeros(acc_ref.shape, f32)

    def add_up(n, total):
        acc_ref[n] = total if pairs == 1 else acc_ref[n] + total

    def unmix(k, d_scale):
        rows = step_rows(k)
        for pr in range(2):
            weighted = []
            for pc in range(2):
                plane = pr * 2 + pc
                share = inv_ref[plane, rows]
                normal = affine(mix_ref[plane, rows], *normal2)
                back = affine(low_ref[plane, rows], back_gain2, back_mean2)
                back = back - scaled(normal, back_normal2)
                d_mixed = jnp.where(share > 0.0, zed_ref[plane, rows] + back, 0.0)
                dx_ref[plane, rows] = d_mixed
                d_scale = d_scale + fold(pool_ref[plane, rows] * d_mixed)
                weighted.append(scale1 * d_mixed * share)
            put_col_windows(col_ref, pr, k, *weighted)
        return d_scale

    add_up(2, sweep(unmix, nothing))
    normal1 = (spread(scaling1, C2), spread(-mean1 * scaling1, C2))

    def unpool(k, carry):
        d_shift, d_gain = carry
        rows = step_rows(k)
        for pc in range(2):
            windows = row_windows(col_ref, pc, k)
            for pr in range(2):
                plane = pr * 2 + pc
                valid = inv_ref[plane, rows] > 0.0
                d_normal = windows[pr] - scale1 * dx_ref[plane, rows]
                d_normal = jnp.where(valid, d_normal, 0.0)
                back_ref[plane, rows] = d_normal
                normal = affine(x_ref[plane, rows], *normal1)
                d_shift = d_shift + fold(d_normal)
                d_gain = d_gain + fold(d_normal * normal)
        return (d_shift, d_gain)

    d_shift, d_gain = sweep(unpool, (nothing, nothing))
    add_up(1, d_shift)
    add_up(0, d_gain)
    mean_shift = by_image(d_shift * gain1) / count_two
    mean_gain = by_image(d_gain * gain1) / count_two
    back_gain1 = scaling1 * gain1
    back_mean1 = spread(-scaling1 * mean_shift, C2)
    back_normal1 = spread(scaling1 * mean_gain, C2)

    def unnorm(k, carry):
        rows = step_rows(k)
        for plane in range(4):
            normal = affine(x_ref[plane, rows], *normal1)
            back = affine(back_ref[plane, rows], back_gain1, back_mean1)
            back = back - scaled(normal, back_normal1)
            valid = inv_ref[plane, rows] > 0.0
            dx_ref[plane, rows] = jnp.where(valid, dx_ref[plane, rows] + back, 0.0)
        return carry

    sweep(unnorm, 0)

    def give_back(image, plane, line_place, there):
        image_ref[image, there] = dx_ref[plane, line_place]

    image_ref[...] = jnp.zeros(image_ref.shape, f32)
    each_image(size_ref, pair, give_back)

    def from_rows(within, carry):
        for spot in range(2 * STRIPS):
            image, strip = spot // STRIPS, spot % STRIPS
            start = pl.multiple_of((strip * SR + within) * LINE, LINE)
            target = strip_place(pair, spot, strip_count)
            payload_ref[target, within] = image_ref[image, pl.ds(start, CW)].astype(bf16)
        return carry

    lax.fori_loop(0, SR, from_rows, 0)

    def finish():
        copy = pltpu.make_async_copy(payload_ref, payload_hbm, sem)
        copy.start()
        vector_ref[...] = flat_ref[...]
        for n in range(3):
            vector_ref[n : n + 1] = jnp.sum(acc_ref[n], axis=0, keepdims=True)
        copy.wait()

    if pairs == 1:
        finish()
    else:
        pl.when(pair == pairs - 1)(finish)


def run_exit(sizes, state, back, flat, vec_two, strip_count):
    pairs = strip_count // 8
    payload = (strip_count, SR, CW, C2)
    make = pltpu.VMEM if pairs == 1 else jax.ShapeDtypeStruct
    plane_f32 = pltpu.VMEM((4, AREA, C2), f32)
    arrays = [*state, *back]
    if pairs == 1:
        arrays = held_in(pltpu.VMEM, *arrays)
    return pl.pallas_call(
        functools.partial(exit_kernel, pairs, strip_count),
        grid=() if pairs == 1 else (pairs,),
        in_specs=[SMEM]
        + pair_specs(pairs, STATE + BACK, pl.Buffered(1))
        + whole_specs(pairs, [flat.shape, vec_two.shape]),
        out_specs=[HBM] + whole_specs(pairs, [flat.shape]),
        out_shape=[pltpu.HBM(payload, bf16), make(flat.shape, f32)],
        scratch_shapes=[
            pltpu.VMEM(payload, bf16),
            pltpu.VMEM((2, CH * LINE, C2), f32),
            pltpu.VMEM((4, AREA + 2 * LINE, C2), f32),
            plane_f32,
            plane_f32,
            pltpu.VMEM((3, 8, C2), f32),
            pltpu.SemaphoreType.DMA,
        ],
        compiler_params=roomy(8 if pairs == 1 else 40),
        name="exit",
    )(sizes, *arrays, flat, vec_two)


def pack_kernel(master_ref, dense_ref):
    values = master_ref[...]
    dense_ref[...] = jnp.concatenate([values[:, :HALF], values[:, HALF:]], axis=2).astype(bf16)


def pack(master):
    owned = master.shape[0]
    return pl.pallas_call(
        pack_kernel,
        out_shape=jax.ShapeDtypeStruct((owned, HALF, 2 * BS), bf16),
        name="pack",
    )(master)


def fold_pair_kernel(near_ref, got_ref, own_ref, *part_refs):
    share = own_ref.shape[0]

    def one(n, carry):
        for k in range(len(part_refs) + 1):
            total = near_ref[k * share + n].astype(f32) + got_ref[k * share + n].astype(f32)
            if k == 0:
                own_ref[n] = total
            else:
                part_refs[k - 1][n] = total.astype(bf16)
        return carry

    lax.fori_loop(0, share, one, 0, unroll=4)


def fold_pair(near, got, groups):
    shape = ((near.shape[0] - 1) // groups,) + near.shape[1:]
    return pl.pallas_call(
        fold_pair_kernel,
        in_specs=[VMEM_BLOCK] * 2,
        out_specs=[VMEM_BLOCK] * groups,
        out_shape=[pltpu.VMEM(shape, f32)] + [pltpu.VMEM(shape, bf16)] * (groups - 1),
        compiler_params=roomy(4),
        name="fold_pair",
    )(*held_in(pltpu.VMEM, near, got))


def fold_tile_kernel(pieces, spot_ref, *refs):
    piece_refs, refs = refs[:pieces], refs[pieces:]
    vector_refs, refs = refs[:pieces], refs[pieces:]
    out_refs, sum_ref = refs[:-1], refs[-1]
    groups = len(out_refs)
    share = out_refs[0].shape[0]
    owned = piece_refs[0].shape[0]
    total = vector_refs[0][...]
    for ref in vector_refs[1:]:
        total = total + ref[...]
    for n in range(sum_ref.shape[0]):
        sum_ref[n] = jnp.zeros((HALF, 128), f32)
    for n in range(VEC_BLOCKS):
        sum_ref[n] = total[n * HALF : (n + 1) * HALF]

    def one(n, carry):
        for k, out_ref in enumerate(out_refs):
            number = lax.rem(spot_ref[0] + k, groups) * share + n
            block = jnp.minimum(number, owned - 1)
            total = piece_refs[0][block].astype(f32)
            for ref in piece_refs[1:]:
                total = total + ref[block].astype(f32)
            rest = sum_ref[jnp.maximum(number - owned, 0)]
            out_ref[n] = jnp.where(number < owned, total, rest).astype(out_ref.dtype)
        return carry

    lax.fori_loop(0, share, one, 0, unroll=share <= 16)


def fold_tile(spot, pieces, vectors, extra, groups):
    shape = ((pieces[0].shape[0] + extra) // groups,) + pieces[0].shape[1:]
    return pl.pallas_call(
        functools.partial(fold_tile_kernel, len(pieces)),
        in_specs=[SMEM] + [VMEM_BLOCK] * (len(pieces) + len(vectors)),
        out_specs=[VMEM_BLOCK] * groups,
        out_shape=[pltpu.VMEM(shape, f32)] + [pltpu.VMEM(shape, bf16)] * (groups - 1),
        scratch_shapes=[pltpu.VMEM((extra, HALF, 128), f32)],
        compiler_params=roomy(8),
        name="fold_tile",
    )(spot, *held_in(pltpu.VMEM, *pieces, *vectors))


def fold_batch_kernel(owned, vector_weight, spot_ref, *refs):
    part_refs, (total_ref, norm_ref) = refs[:-2], refs[-2:]
    share = total_ref.shape[0]
    square = jnp.zeros((8, 128), f32)
    for n in range(share):
        total = part_refs[0][n].astype(f32)
        for ref in part_refs[1:]:
            total = total + ref[n].astype(f32)
        total_ref[n] = total.astype(bf16)
        weight = jnp.where(spot_ref[0] * share + n < owned, 1.0, vector_weight)
        square = square + weight * fold(total * total)
    square = jnp.sum(jnp.sum(square, axis=1, keepdims=True), axis=0, keepdims=True)
    norm_ref[...] = jnp.broadcast_to(square[None], norm_ref.shape)


def fold_batch(spot, parts, owned, tile_count):
    count = tile_count * len(parts)
    return pl.pallas_call(
        functools.partial(fold_batch_kernel, owned, 1.0 / tile_count),
        in_specs=[SMEM] + [VMEM_BLOCK] * len(parts),
        out_specs=[VMEM_BLOCK] * 2,
        out_shape=[pltpu.VMEM(parts[0].shape, bf16), pltpu.VMEM((count, 1, 128), f32)],
        name="fold_batch",
    )(spot, *held_in(pltpu.VMEM, *parts))


def update_kernel(owned, groups, spot_ref, norm_ref, *refs):
    quarters, refs = refs[:groups], refs[groups:]
    stat_hbm, out_hbm, (vector_ref, clip_ref), refs = refs[:5], refs[5:10], refs[10:12], refs[12:]
    stat_refs, out_refs, (in_sem, out_sem) = refs[:5], refs[5:10], refs[10:]
    master_ref, left_stat_ref, right_stat_ref, left_root_ref, right_root_ref = stat_refs
    grad_ref, left_ref, right_ref, new_ref, copy_ref = out_refs
    share = quarters[0].shape[0]
    spans = spans_of(owned)

    def copies_of(sources, targets, sems):
        return [
            [
                pltpu.make_async_copy(
                    source.at[pl.ds(*span)], target.at[pl.ds(*span)], sems.at[5 * n + k]
                )
                for k, (source, target) in enumerate(zip(sources, targets))
            ]
            for n, span in enumerate(spans)
        ]

    copies_in = copies_of(stat_hbm, stat_refs, in_sem)
    copies_out = copies_of(out_refs, out_hbm, out_sem)
    for copies in copies_in:
        for copy in copies:
            copy.start()
    norm = jnp.sqrt(jnp.sum(norm_ref[...], axis=0))
    factor = jnp.minimum(1.0, clip_limit / norm)
    left_half = lax.broadcasted_iota(jnp.int32, (HALF, 128), 1) < BS

    def summed(number):
        source = number // share
        local = number - source * share
        turn = lax.rem(spot_ref[0] - source + groups, groups)
        value = quarters[0][local].astype(f32)
        for k in range(1, groups):
            value = jnp.where(turn == k, quarters[k][local].astype(f32), value)
        return value * factor

    def side_by_side(first, count):
        sides = []
        for n in range(first, first + count, 2):
            dense = summed(n)
            turned = pltpu.roll(dense, BS, 1)
            if n + 1 < first + count:
                second = summed(n + 1)
                top = jnp.where(left_half, dense, pltpu.roll(second, BS, 1))
                low = jnp.where(left_half, turned, second)
                side = jnp.concatenate([top, low], axis=0)
                grad_ref[n + 1] = pltpu.roll(side, BS, 1)[:, :BS]
            else:
                side = jnp.concatenate([dense, turned], axis=0)[:, :BS]
            grad_ref[n] = side[:, :BS]
            sides.append(side.astype(bf16))
        return jnp.concatenate(sides, axis=1)

    def diagonal_of(count):
        order = (count * BS, count * BS)
        return lax.broadcasted_iota(jnp.int32, order, 0) // BS == (
            lax.broadcasted_iota(jnp.int32, order, 1) // BS
        )

    clip_ref[...] = norm
    for n in range(vector_ref.shape[0]):
        vector_ref[n] = summed(owned + n)
    for (first, length), arriving, leaving in zip(spans, copies_in, copies_out):
        parts = [(n, min(4, first + length - n)) for n in range(first, first + length, 4)]
        wides = [side_by_side(*part) for part in parts]
        tall = [
            jnp.where(diagonal_of(count), jnp.concatenate([wide] * count, axis=0), 0.0)
            for (_, count), wide in zip(parts, wides)
        ]
        lefts = [product_nt(one, wide) for one, wide in zip(tall, wides)]
        rights = [product_tn(wide, wide) for wide in wides]
        for copy in arriving:
            copy.wait()
        stepped = []
        for (start, count), wide in zip(parts, wides):
            roots = left_root_ref[pl.ds(start, count)].reshape(count * BS, BS).astype(bf16)
            stepped.append(product(roots, wide))
        for (start, count), left, right in zip(parts, lefts, rights):
            here = pl.ds(start, count)
            left_ref[here] = 0.5 * left_stat_ref[here] + 0.5 * left.reshape(count, BS, BS)
            for n in range(count):
                at = n // 2 * 128
                block = right[n * BS : n * BS + BS, at : min(at + 128, count * BS)]
                if n % 2:
                    block = pltpu.roll(block, BS, 1)
                right_ref[start + n] = 0.5 * right_stat_ref[start + n] + 0.5 * block[:, :BS]
        for (start, count), value in zip(parts, stepped):
            here = pl.ds(start, count)
            value = jnp.where(diagonal_of(count), value, 0.0).astype(bf16)
            roots = right_root_ref[here].reshape(count * BS, BS).astype(bf16)
            value = product(value, roots).reshape(count, BS, BS)
            new = master_ref[here] - rate_matrix * value
            new_ref[here] = new
            copy_ref[here] = new.astype(bf16)
        for copy in leaving:
            copy.start()
    for leaving in copies_out:
        for copy in leaving:
            copy.wait()


def spans_of(owned):
    spans = []
    first = 0
    while first < owned:
        length = min(8 if first == 0 else 12, owned - first)
        spans.append((first, length))
        first += length
    return spans


def update(spot, norm, quarters, extra, *stats):
    shape = stats[0].shape
    groups = len(quarters)
    types = [f32] * 4 + [bf16]
    steps = len(spans_of(shape[0]))
    return pl.pallas_call(
        functools.partial(update_kernel, shape[0], groups),
        in_specs=[SMEM] + [VMEM_BLOCK] * (groups + 1) + [HBM] * 5,
        out_specs=[HBM] * 5 + [VMEM_BLOCK] * 2,
        out_shape=[pltpu.HBM(shape, kind) for kind in types]
        + [
            pltpu.VMEM((extra, HALF, 128), f32),
            pltpu.VMEM((1, 128), f32),
        ],
        scratch_shapes=[pltpu.VMEM(shape, f32)] * 5
        + [pltpu.VMEM(shape, kind) for kind in types]
        + [
            pltpu.SemaphoreType.DMA((5 * steps,)),
            pltpu.SemaphoreType.DMA((5 * steps,)),
        ],
        compiler_params=roomy(20),
        name="update",
    )(spot, *held_in(pltpu.VMEM, norm, *quarters), *held_in(pltpu.HBM, *stats))


def share_out(pieces, axis):
    return lax.all_to_all(pieces, axis, split_axis=0, concat_axis=0, tiled=True)


def swap(piece, distance):
    count = lax.axis_size("tile")
    return lax.ppermute(piece, "tile", [(i, i ^ distance) for i in range(count)])


def on_device(
    pixels,
    buckets,
    slot_owner_table,
    out_grad,
    master,
    left_stat,
    right_stat,
    left_root,
    right_root,
    vectors,
    moment,
):
    tile_count = lax.axis_size("tile")
    tile_place = lax.axis_index("tile")
    slot_count = pixels.shape[2]
    group_count = tile_count // STRIPS
    pairs = group_count // 2
    owned = master.shape[0]
    slots = owned * tile_count
    batch_count = lax.axis_size("batch")
    spot = lax.axis_index("batch").astype(jnp.int32).reshape(1)
    extra = extra_of(owned, batch_count)
    strips = share_out(pixels.reshape((tile_count,) + pixels.shape[3:]), "tile")
    dense = pack(master)
    paired = tile_count <= 8
    if paired:
        mine = [dense] + [swap(dense, 2 * k) for k in range(1, tile_count // 2)]
        pieces = mine + [swap(piece, 1) for piece in mine]
    else:
        pieces = [lax.all_gather(dense, "tile", axis=0, tiled=True)]

    numbers = jnp.arange(slots, dtype=jnp.int32)
    slot_of = jnp.sum(
        jnp.where(slot_owner_table[None, :] == numbers[:, None], numbers[None, :], 0), axis=1
    )
    owner = slot_of // owned
    within = slot_of - owner * owned
    place_of = slot_of
    if paired:
        apart = owner ^ tile_place
        apart = (apart & 1) * (tile_count // 2) + (apart >> 1)
        slot_of = place_of = within + owned * apart
    half = slots // 2
    near_place = jnp.where(place_of < half, place_of, half)
    far_place = jnp.where(place_of < half, half, place_of - half)
    image_ids = lax.dynamic_index_in_dim(
        buckets.reshape(group_count, slot_count), tile_place, 1, keepdims=False
    )
    turned = image_ids >= 2
    heights = jnp.where(image_ids == 0, 5 * CH // 9, jnp.where(image_ids == 1, 7 * CH // 9, CH))
    breadths = jnp.where(image_ids == 0, CW, jnp.where(image_ids == 1, 7 * CW // 9, 5 * CW // 9))
    sizes = jnp.stack(
        [
            jnp.where(turned, breadths, heights),
            jnp.where(turned, heights, breadths),
            turned,
        ],
        axis=1,
    )
    sizes = sizes.reshape(-1).astype(jnp.int32)

    two = 6 * C2 + HID2 + C2
    vec_two = jnp.concatenate([vectors[: 6 * C2], vectors[6 * C2 + HID2 : two]]).reshape(7, C2)
    vec_hid_two = vectors[6 * C2 : 6 * C2 + HID2].reshape(1, HID2)
    wide_end = two + 7 * C3
    vec_three = jnp.concatenate([vectors[two:wide_end], vectors[wide_end + HID3 :]])
    vec_three = jnp.pad(vec_three.reshape(8, C3), ((0, 0), (0, WIDE - C3)))
    vec_hid_three = vectors[wide_end : wide_end + HID3].reshape(1, HID3)

    flips = turned.reshape(-1, 1, 1, 1)
    goal = out_grad.reshape(2 * pairs, H3, W3, C3)
    goal = jnp.where(flips, goal.transpose(0, 2, 1, 3), goal)[:, :LINES]
    goal = goal.reshape(pairs, 2, LINES, W3, C3).transpose(0, 2, 3, 1, 4)
    goal = goal.reshape(pairs, LINES, 2 * W3, C3)
    goal = jnp.pad(goal, ((0, 0), (0, 0), (0, LINE - 2 * W3), (0, WIDE - C3)))
    goal = goal.reshape(pairs, AREA, WIDE)

    weights = run_unpack(slot_of, pieces)
    strips, *weights = lax.optimization_barrier((strips, *weights))
    state = run_entry(sizes, strips, vec_two)
    result, *back, near, far, flat = run_main(
        (near_place, far_place),
        sizes,
        state,
        goal,
        (vec_two, vec_hid_two, vec_three, vec_hid_three),
        weights,
        tile_count,
    )
    pixel_back, vector = run_exit(sizes, state, back, flat, vec_two, tile_count)
    if paired:
        own, *parts = fold_pair(near, swap(far, 1), tile_count // 2)
        pieces = [own] + [swap(part, 2 * k + 2) for k, part in enumerate(parts)]
        vector, _ = lax.optimization_barrier((vector, parts[0]))
        vector = vector + swap(vector, 1)
        vectors_in = [vector] + [swap(vector, 2 * k) for k in range(1, tile_count // 2)]
    else:
        outgoing = jnp.concatenate([near[:half], far[:half]], axis=0)
        pieces = list(share_out(outgoing.reshape(tile_count, owned, HALF, 128), "tile"))
        vectors_in = list(lax.all_gather(vector, "tile"))
    result, pieces[1] = lax.optimization_barrier((result, pieces[1]))
    result = result.reshape(pairs, LINES, LINE, WIDE)[:, :, : 2 * W3, :C3]
    result = result.reshape(pairs, LINES, W3, 2, C3).transpose(0, 3, 1, 2, 4)
    result = result.reshape(2 * pairs, LINES, W3, C3)
    result = jnp.pad(result, ((0, 0), (0, H3 - LINES), (0, 0), (0, 0)))
    result = jnp.where(flips, result.transpose(0, 2, 1, 3), result)
    result = result.reshape(out_grad.shape)
    result = with_layout_constraint(result, Layout(major_to_minor=(0, 1, 2, 4, 5, 3, 6)))
    result, vectors_in[0] = lax.optimization_barrier((result, vectors_in[0]))
    own, *parts = fold_tile(spot, pieces, vectors_in, extra, batch_count)
    pixel_back, parts[0] = lax.optimization_barrier((pixel_back, parts[0]))
    returned = share_out(pixel_back, "tile")
    parts = [
        lax.ppermute(part, "batch", [(i, (i + k + 1) % batch_count) for i in range(batch_count)])
        for k, part in enumerate(parts)
    ]
    quarter, norm = fold_batch(spot, [own] + parts, owned, tile_count)
    returned, norm = lax.optimization_barrier((returned, norm))
    norm = share_out(norm, ("batch", "tile"))
    returned = returned.astype(f32).reshape(pixels.shape)
    returned = with_layout_constraint(returned, Layout(major_to_minor=(0, 1, 3, 4, 2, 5)))
    returned, quarter = lax.optimization_barrier((returned, quarter))
    quarters = [quarter] + [
        lax.ppermute(quarter, "batch", [(i, (i + k) % batch_count) for i in range(batch_count)])
        for k in range(1, batch_count)
    ]
    block_grad, left_new, right_new, master_new, weight_copy, whole_vector, clip = update(
        spot, norm, quarters, extra, master, left_stat, right_stat, left_root, right_root
    )
    clip_norm = clip[0, 0]
    share = vectors.shape[0] // tile_count
    whole_vector = whole_vector.reshape(-1)
    vec_grad = lax.dynamic_slice_in_dim(whole_vector, tile_place * share, share, 0)
    vec_moment = moment + vec_grad * vec_grad
    own_vectors = lax.dynamic_slice_in_dim(vectors, tile_place * share, share, 0)
    vec_new = own_vectors - rate_vector * vec_grad / (jnp.sqrt(vec_moment) + eps_adagrad)
    return (
        result,
        returned,
        clip_norm,
        block_grad,
        left_new,
        right_new,
        master_new,
        weight_copy,
        vec_grad,
        vec_moment,
        vec_new,
    )


def solution(mesh):
    placed = (
        P("batch", "tile", None, None, None, None),
        P("batch"),
        P(),
        P("batch", "tile", None, None, None, None, None),
        P("tile", None, None),
        P("tile", None, None),
        P("tile", None, None),
        P("tile", None, None),
        P("tile", None, None),
        P(),
        P("tile"),
    )
    return jax.shard_map(
        on_device,
        mesh=mesh,
        in_specs=placed,
        out_specs=(
            P("batch", "tile", None, None, None, None, None),
            P("batch", "tile", None, None, None, None),
            P(),
            P("tile", None, None),
            P("tile", None, None),
            P("tile", None, None),
            P("tile", None, None),
            P("tile", None, None),
            P("tile"),
            P("tile"),
            P("tile"),
        ),
        check_vma=False,
    )
```

```python
import functools

import jax
import jax.numpy as jnp
from jax import lax
from jax.experimental import pallas as pl
from jax.experimental.layout import Layout, with_layout_constraint
from jax.experimental.pallas import tpu as pltpu
from jax.sharding import PartitionSpec as P

C2 = 128
HID2 = 512
C3 = 320
HID3 = 1280
CH = 36
CW = 36
STRIPS = 4
BS = 64
SR = CH // STRIPS
H3 = CH // 2
W3 = CW // 2
LONG = 7 * CH // 9
LINES = LONG // 2
WIDE = 384
LINE = 40
AREA = LINES * LINE
STEP = 2 * LINE
STEPS = AREA // STEP
HALF = BS // 2
STRIP = SR * CW
STRIP_ROWS = STRIP + -STRIP % 16

eps_norm = 1e-05
clip_limit = 1.0
rate_matrix = 0.3
rate_vector = 0.3
eps_adagrad = 1e-08
f32 = jnp.float32
bf16 = jnp.bfloat16

SHAPES = [(C2, HID2), (HID2, C2), (9 * C2, C3), (C3, HID3), (HID3, C3)]
USED = sum(rows // BS * (cols // BS) for rows, cols in SHAPES)
VEC_ROWS = (6 * C2 + HID2 + C2 + C3 + 6 * C3 + HID3 + C3) // 128


VEC_BLOCKS = -(-VEC_ROWS // HALF)


def extra_of(owned, groups):
    return VEC_BLOCKS + -(owned + VEC_BLOCKS) % groups


def product(left, right):
    return jnp.dot(left, right, preferred_element_type=f32)


def product_nt(left, right):
    return lax.dot_general(left, right, (((1,), (1,)), ((), ())), preferred_element_type=f32)


def product_tn(left, right):
    return lax.dot_general(left, right, (((0,), (0,)), ((), ())), preferred_element_type=f32)


def gelu_pair(values):
    bell = jnp.exp2(values * values * (-0.5 * 1.4426950408889634))
    step = pl.reciprocal(1.0 + (0.3275911 * 0.7071067811865476) * jnp.abs(values), approx=True)
    tail = step * (
        0.5 * 0.254829592
        + step
        * (
            0.5 * -0.284496736
            + step
            * (0.5 * 1.421413741 + step * (0.5 * -1.453152027 + step * (0.5 * 1.061405429)))
        )
    )
    tail = tail * bell
    share = jnp.where(values >= 0.0, 1.0 - tail, tail)
    return (values * share, share + values * (bell * 0.3989422804014327))


def fold(values):
    chans = values.shape[-1]
    return jnp.sum(values.reshape(-1, 8, chans), axis=0)


def by_image(total):
    total = total + pltpu.roll(total, 4, 0)
    total = total + pltpu.roll(total, 2, 0)
    return jnp.sum(total, axis=1, keepdims=True)


def line(pattern):
    return jnp.concatenate([pattern] * (LINE // 8), axis=0)


def spread(pattern, chans):
    return jnp.broadcast_to(pattern, (8, chans))


def affine(values, factor, shift):
    tiles = values.reshape(-1, 8, values.shape[-1])
    return (tiles * factor + shift).reshape(values.shape)


def scaled(values, factor):
    tiles = values.reshape(-1, 8, values.shape[-1])
    return (tiles * factor).reshape(values.shape)


def from_left(values):
    return pltpu.roll(values, 2, 0)


def from_right(values):
    return pltpu.roll(values, values.shape[0] - 2, 0)


def rounded(values):
    return values.astype(bf16).astype(f32)


def widen(values):
    return jnp.concatenate([values] * (WIDE // 128), axis=-1)


def norm_terms(total, square, count):
    mean = by_image(total) / count
    scaling = lax.rsqrt(by_image(square) / count - mean * mean + eps_norm)
    return (mean, scaling)


def sweep(visit, start):
    return lax.fori_loop(0, STEPS, visit, start, unroll=True)


def step_rows(k, lines=0):
    start = k * STEP + lines * LINE
    return pl.ds(start if isinstance(k, int) else pl.multiple_of(start, LINE), STEP)


def held_in(space, *arrays):
    return [pltpu.with_memory_space_constraint(array, space) for array in arrays]


VMEM_BLOCK = pl.BlockSpec(memory_space=pltpu.VMEM)
HBM = pl.BlockSpec(memory_space=pltpu.HBM)
SMEM = pl.BlockSpec(memory_space=pltpu.SMEM)


def roomy(mebibytes):
    return pltpu.CompilerParams(vmem_limit_bytes=mebibytes * 1024 * 1024)


class Geometry:
    def __init__(self, size_ref, pair):
        parity = lax.broadcasted_iota(jnp.int32, (8, 128), 0) % 2
        high, broad, turned = (
            jnp.where(parity == 0, size_ref[pair * 6 + n], size_ref[pair * 6 + 3 + n])
            for n in range(3)
        )
        self.high = high
        self.count_two = (high * broad * C2).astype(f32)[:, :1]
        self.high3 = (high + 1) // 2
        broad3 = (broad + 1) // 2
        self.count_three = (self.high3 * broad3 * C3).astype(f32)[:, :1]
        place = lax.broadcasted_iota(jnp.int32, (LINE, 128), 0) // 2
        inside = lax.broadcasted_iota(jnp.int32, (LINE, 128), 0) < 2 * W3
        self.reach = []
        self.col_share = []
        for pc in range(2):
            column = 2 * place + pc
            self.reach.append(jnp.where(inside & (column < line(broad)), line(high), 0))
            edge = (column == 0) | (column == line(broad) - 1)
            self.col_share.append(jnp.where(edge, 0.5, 1.0 / 3.0))
        self.reach3 = jnp.where(inside & (place < line(broad3)), line(self.high3), 0)
        edge3 = (place == 0) | (place == line(broad3) - 1)
        self.col_share3 = jnp.where(edge3, 0.5, 1.0 / 3.0)
        self.flipped = jnp.concatenate([turned] * (STEP // 8), axis=0) > 0

    def share(self, plane, k):
        pr, pc = plane // 2, plane % 2
        return self.lines(4 * k + pr, 2, self.reach[pc], self.col_share[pc], self.high)

    def share3(self, k):
        return self.lines(2 * k, 1, self.reach3, self.col_share3, self.high3)

    def lines(self, row, stride, reach, col_share, height):
        parts = []
        for n in range(2):
            here = row + stride * n
            row_share = jnp.where((here == 0) | (here == height - 1), 0.5, 1.0 / 3.0)
            parts.append(jnp.where(here < reach, line(row_share) * col_share, 0.0))
        return jnp.concatenate(parts, axis=0)


def strip_place(pair, spot, strip_count):
    return lax.rem(pair * 8 + strip_count - 2 + spot, strip_count)


def each_image(size_ref, pair, visit):
    for image in range(2):
        way = size_ref[pair * 6 + 3 * image + 2]

        @pl.when(way == 0)
        def _():
            def one(r, carry):
                for plane in range(4):
                    row = 2 * r + plane // 2
                    strip = row // SR
                    there = pl.ds((row - strip * SR) * CW + plane % 2, W3, stride=2)
                    here = pl.ds(r * LINE + image, W3, stride=2)
                    visit(plane, here, image * STRIPS + strip, there)
                return carry

            lax.fori_loop(0, LINES, one, 0)

        @pl.when(way == 1)
        def _():
            def one(r, carry):
                for plane in range(4):
                    for strip in range(STRIPS):
                        first = (plane % 2 + strip * SR) % 2
                        count = (SR - first + 1) // 2
                        done = (strip * SR + first) // 2
                        column = 2 * r + plane // 2
                        there = pl.ds(first * CW + column, count, stride=2 * CW)
                        here = pl.ds(r * LINE + image + 2 * done, count, stride=2)
                        visit(plane, here, image * STRIPS + strip, there)
                return carry

            lax.fori_loop(0, LINES, one, 0)


def row_windows(col_ref, pc, k):
    both = col_ref[pc, step_rows(k, 1)] + col_ref[2 + pc, step_rows(k, 1)]
    return (both + col_ref[2 + pc, step_rows(k)], both + col_ref[pc, step_rows(k, 2)])


def put_col_windows(col_ref, pr, k, even, odd):
    both = even + odd
    col_ref[pr * 2, step_rows(k, 1)] = both + from_left(odd)
    col_ref[pr * 2 + 1, step_rows(k, 1)] = both + from_right(even)


def clear_edges(col_ref):
    zero_line = jnp.zeros((LINE, C2), f32)
    for plane in range(4):
        col_ref[plane, 0:LINE] = zero_line
        col_ref[plane, AREA + LINE : AREA + 2 * LINE] = zero_line


def entry_kernel(pairs, strip_count, piece_count, place_ref, size_ref, vec_two_ref, *refs):
    piece_refs, refs = refs[:piece_count], refs[piece_count:]
    x_out, inv_out, pool_out, mix_out, stat_out, image_ref, col_ref = refs
    pair = pl.program_id(0) if pairs > 1 else 0
    x_ref, inv_ref, pool_ref, mix_ref = (ref.at[0] for ref in (x_out, inv_out, pool_out, mix_out))
    shape = Geometry(size_ref, pair)
    gain1, bias1, scale1 = (vec_two_ref[n : n + 1] for n in range(3))
    clear_edges(col_ref)
    if piece_count > 1:
        half = piece_count // 2
        for n, ref in enumerate(piece_refs):
            source = place_ref[0] ^ (n // half + 2 * (n % half))
            spot = lax.rem(source + 2, 2 * STRIPS)
            first = 0 if n < half else ref.shape[0] - STRIP_ROWS
            image_ref[spot] = ref[first : first + STRIP_ROWS].astype(f32)
    else:
        for spot in range(2 * STRIPS):
            source = strip_place(pair, spot, strip_count)
            image_ref[spot] = piece_refs[0][source].astype(f32)

    def take_in(plane, here, spot, there):
        x_ref[plane, here] = image_ref[spot, there]

    each_image(size_ref, pair, take_in)

    def arrange(k, carry):
        total, square = carry
        rows = step_rows(k)
        for plane in range(4):
            share = shape.share(plane, k)
            inv_ref[plane, rows] = share
            values = jnp.where(share > 0.0, x_ref[plane, rows], 0.0)
            x_ref[plane, rows] = values
            total = total + fold(values)
            square = square + fold(values * values)
        return (total, square)

    nothing = jnp.zeros((8, C2), f32)
    total, square = sweep(arrange, (nothing, nothing))
    mean1, scaling1 = norm_terms(total, square, shape.count_two)
    factor1 = scaling1 * gain1
    shift1 = bias1 - mean1 * scaling1 * gain1

    def window_cols(k, carry):
        rows = step_rows(k)
        for pr in range(2):
            masked = []
            for pc in range(2):
                plane = pr * 2 + pc
                normal = rounded(affine(x_ref[plane, rows], factor1, shift1))
                masked.append(jnp.where(inv_ref[plane, rows] > 0.0, normal, 0.0))
            put_col_windows(col_ref, pr, k, *masked)
        return carry

    sweep(window_cols, 0)

    def mix(k, carry):
        total, square = carry
        rows = step_rows(k)
        for pc in range(2):
            windows = row_windows(col_ref, pc, k)
            for pr in range(2):
                plane = pr * 2 + pc
                values = x_ref[plane, rows]
                share = inv_ref[plane, rows]
                pooled = windows[pr] * share - rounded(affine(values, factor1, shift1))
                pooled = jnp.where(share > 0.0, pooled, 0.0)
                mixed = values + scale1 * pooled
                pool_ref[plane, rows] = pooled
                mix_ref[plane, rows] = mixed
                total = total + fold(mixed)
                square = square + fold(mixed * mixed)
        return (total, square)

    total, square = sweep(mix, (nothing, nothing))
    mean2, scaling2 = norm_terms(total, square, shape.count_two)
    for n, value in enumerate((mean1, scaling1, mean2, scaling2)):
        stat_out[0, n] = spread(value, 128)


def pair_specs(pairs, shapes, mode=None):
    if pairs == 1:
        return [VMEM_BLOCK] * len(shapes)
    return [
        pl.BlockSpec(
            (1,) + shape, lambda t, rank=len(shape): (t,) + (0,) * rank, pipeline_mode=mode
        )
        for shape in shapes
    ]


def whole_specs(pairs, shapes):
    if pairs == 1:
        return [VMEM_BLOCK] * len(shapes)
    return [
        pl.BlockSpec(
            shape,
            lambda t, rank=len(shape): (0,) * rank,
            pipeline_mode=pl.Buffered(1),
        )
        for shape in shapes
    ]


def pair_arrays(pairs, shapes, kinds):
    make = pltpu.VMEM if pairs == 1 else jax.ShapeDtypeStruct
    return [make((pairs,) + shape, kind) for shape, kind in zip(shapes, kinds)]


STATE = [(4, AREA, C2)] * 4 + [(4, 8, 128)]
BACK = [(4, AREA, C2)] * 2 + [(2, 8, 128)]


def run_entry(place, sizes, pieces, vec_two, strip_count):
    pairs = strip_count // 8
    if pairs == 1:
        pieces = held_in(pltpu.VMEM, *pieces)
    return pl.pallas_call(
        functools.partial(entry_kernel, pairs, strip_count, len(pieces)),
        grid=() if pairs == 1 else (pairs,),
        in_specs=[SMEM] * 2 + whole_specs(pairs, [array.shape for array in (vec_two, *pieces)]),
        out_specs=pair_specs(pairs, STATE),
        out_shape=pair_arrays(pairs, STATE, [f32] * 5),
        scratch_shapes=[
            pltpu.VMEM((2 * STRIPS, STRIP_ROWS, C2), f32),
            pltpu.VMEM((4, AREA + 2 * LINE, C2), f32),
        ],
        compiler_params=roomy(6 if pairs == 1 else 40),
        name="entry",
    )(place, sizes, vec_two, *pieces)


WEIGHTS = [(C2, HID2), (HID2, C2), (9 * C2, WIDE), (WIDE, HID3), (HID3, WIDE)]


def unpack_kernel(piece_count, slot_ref, *refs):
    piece_refs, refs = refs[:piece_count], refs[piece_count:]
    weights, gathered_ref = refs[:-1], refs[-1]
    count = gathered_ref.shape[0] // piece_count
    first = STRIP_ROWS if piece_count > 1 else 0
    for n, ref in enumerate(piece_refs):
        blocks = ref[first : first + count * HALF].reshape(count, HALF, 128)
        gathered_ref[n * count : n * count + count] = blocks
    left_half = lax.broadcasted_iota(jnp.int32, (HALF, 128), 1) < BS
    offset = 0
    for (rows, cols), ref in zip(SHAPES, weights):
        wide = cols // BS
        for rb in range(rows // BS):
            for cb in range(0, wide, 2):
                number = offset + rb * wide + cb
                first = gathered_ref[slot_ref[number]]
                turned = pltpu.roll(first, BS, 1)
                if cb + 1 < wide:
                    second = gathered_ref[slot_ref[number + 1]]
                    top = jnp.where(left_half, first, pltpu.roll(second, BS, 1))
                    low = jnp.where(left_half, turned, second)
                else:
                    top = jnp.where(left_half, first, 0.0)
                    low = jnp.where(left_half, turned, 0.0)
                place = slice(cb * BS, cb * BS + 128)
                ref[rb * BS : rb * BS + HALF, place] = top
                ref[rb * BS + HALF : rb * BS + BS, place] = low
        offset += rows // BS * wide
    weights[3][C3:, :] = jnp.zeros((WIDE - C3, HID3), bf16)


def run_unpack(slot_of, pieces):
    slots = slot_of.shape[0]
    return pl.pallas_call(
        functools.partial(unpack_kernel, len(pieces)),
        in_specs=[SMEM] + [VMEM_BLOCK] * len(pieces),
        out_specs=[VMEM_BLOCK] * 5,
        out_shape=[pltpu.VMEM(shape, bf16) for shape in WEIGHTS],
        scratch_shapes=[pltpu.VMEM((slots, HALF, 128), bf16)],
        compiler_params=roomy(6),
        name="unpack",
    )(slot_of, *held_in(pltpu.VMEM, *pieces))


def main_kernel(
    pairs,
    strip_count,
    slots,
    near_place,
    far_place,
    size_ref,
    inv_in,
    mix_in,
    stat_in,
    goal_ref,
    vec_two_ref,
    vec_hid_two_ref,
    vec_three_ref,
    vec_hid_three_ref,
    w1_ref,
    w2_ref,
    we_ref,
    w3_ref,
    w4_ref,
    result_ref,
    zed_out,
    dx_out,
    mean_out,
    near_ref,
    far_ref,
    flat_ref,
    zed_ref,
    hid_ref,
    u_ref,
    g_ref,
    h_ref,
    dy_ref,
    patch_ref,
    dpatch_ref,
    inv3_ref,
    e_ref,
    col3_ref,
    pool3_ref,
    mix3_ref,
    dx3_ref,
    hid3_ref,
    dhid3_ref,
    u3_ref,
    g3_ref,
    h3_ref,
    dy3_ref,
    dpre_ref,
    gw1_ref,
    gw2_ref,
    gwe_ref,
    gw3_ref,
    gw4_ref,
    acc_two,
    acc_hid_two,
    acc_three,
    acc_hid_three,
):
    pair = pl.program_id(0) if pairs > 1 else 0
    grads = [gw1_ref, gw2_ref, gwe_ref, gw3_ref, gw4_ref]
    inv_ref, mix_ref, stat_ref = (ref.at[0] for ref in (inv_in, mix_in, stat_in))
    back_ref, dx_ref = zed_out.at[0], dx_out.at[0]
    left_half = lax.broadcasted_iota(jnp.int32, (HALF, 128), 1) < BS

    def at_pair(number, act):
        if pairs == 1:
            act()
        else:
            pl.when(pair == number)(act)

    def begin():
        acc_two[...] = jnp.zeros(acc_two.shape, f32)
        acc_hid_two[...] = jnp.zeros(acc_hid_two.shape, f32)
        acc_three[...] = jnp.zeros(acc_three.shape, f32)
        acc_hid_three[...] = jnp.zeros(acc_hid_three.shape, f32)

    at_pair(0, begin)
    shape = Geometry(size_ref, pair)
    count_two, count_three, flipped = shape.count_two, shape.count_three, shape.flipped
    nothing = jnp.zeros((8, C2), f32)
    nothing3 = jnp.zeros((8, WIDE), f32)
    gain2, bias2, scale2, out_bias = (vec_two_ref[n : n + 1] for n in range(3, 7))
    embed_bias, gain3, bias3, scale3 = (vec_three_ref[n : n + 1] for n in range(4))
    gain4, bias4, scale4, out_bias3 = (vec_three_ref[n : n + 1] for n in range(4, 8))
    mean2, scaling2 = stat_ref[2], stat_ref[3]
    factor2 = scaling2 * gain2
    shift2 = bias2 - mean2 * scaling2 * gain2
    for plane in range(4):
        zed_ref[plane, 0:LINE] = jnp.zeros((LINE, C2), f32)
    col3_ref[0:LINE] = jnp.zeros((LINE, WIDE), f32)
    col3_ref[AREA + LINE : AREA + 2 * LINE] = jnp.zeros((LINE, WIDE), f32)

    def put_block(number, block):
        near_ref[near_place[number]] = block
        far_ref[far_place[number]] = block

    def pack_blocks(matrices):
        offsets = [0]
        for rows, cols in SHAPES:
            offsets.append(offsets[-1] + rows // BS * (cols // BS))
        for which in matrices:
            (rows, cols), ref = SHAPES[which], grads[which]
            wide = cols // BS
            for rb in range(rows // BS):
                for cb in range(0, wide, 2):
                    number = offsets[which] + rb * wide + cb
                    at = slice(cb * BS, cb * BS + 128)
                    top = ref[rb * BS : rb * BS + HALF, at].astype(bf16)
                    low = ref[rb * BS + HALF : rb * BS + BS, at].astype(bf16)
                    put_block(number, jnp.where(left_half, top, pltpu.roll(low, BS, 1)))
                    if cb + 1 < wide:
                        put_block(number + 1, jnp.where(left_half, pltpu.roll(top, BS, 1), low))

    def plane_rows(plane):
        return slice(plane * AREA, plane * AREA + AREA)

    def begin_plane(plane):
        low = affine(mix_ref[plane], factor2, shift2).astype(bf16)
        h_ref[plane_rows(plane)] = low
        hid_ref[plane % 2] = product(low, w1_ref[...])

    begin_plane(0)
    for plane in range(4):
        if plane < 3:
            begin_plane(plane + 1)
        for k in range(STEPS):
            rows = step_rows(k)
            flat = slice(plane * AREA + k * STEP, plane * AREA + k * STEP + STEP)
            for at in range(0, HID2, 128):
                lanes = slice(at, at + 128)
                active, slope = gelu_pair(hid_ref[plane % 2, rows, lanes] + vec_hid_two_ref[:, lanes])
                u_ref[flat, lanes] = active.astype(bf16)
                g_ref[flat, lanes] = slope.astype(bf16)
        out = product(u_ref[plane_rows(plane)], w2_ref[...]) + out_bias
        zed = jnp.where(inv_ref[plane] > 0.0, mix_ref[plane] + scale2 * out, 0.0)
        zed_ref[plane, LINE : LINE + AREA] = rounded(zed)

    def patches(k, carry):
        rows = step_rows(k)
        taps = []
        for ky in range(3):
            pr = (0 if ky == 1 else 1) * 2
            source = step_rows(k, 0 if ky == 0 else 1)
            even = zed_ref[pr, source]
            odd = zed_ref[pr + 1, source]
            taps.append((from_left(odd), even, odd))
        for ky in range(3):
            for kx in range(3):
                at = (3 * ky + kx) * C2
                tap = taps[ky][kx]
                if ky != kx:
                    tap = jnp.where(flipped, taps[kx][ky], tap)
                patch_ref[rows, at : at + C2] = tap.astype(bf16)
        return carry

    sweep(patches, 0)
    e_ref[...] = product(patch_ref[...], we_ref[...])

    def embed(k, carry):
        total, square = carry
        rows = step_rows(k)
        share = shape.share3(k)
        inv3_ref[rows] = share
        out = jnp.where(widen(share) > 0.0, e_ref[rows] + embed_bias, 0.0)
        e_ref[rows] = out
        return (total + fold(out), square + fold(out * out))

    total, square = sweep(embed, (nothing3, nothing3))
    mean3, scaling3 = norm_terms(total, square, count_three)
    factor3 = scaling3 * gain3
    shift3 = bias3 - mean3 * scaling3 * gain3

    def window_cols3(k, carry):
        rows = step_rows(k)
        normal = rounded(affine(e_ref[rows], factor3, shift3))
        masked = jnp.where(widen(inv3_ref[rows]) > 0.0, normal, 0.0)
        col3_ref[step_rows(k, 1)] = masked + from_left(masked) + from_right(masked)
        return carry

    sweep(window_cols3, 0)

    def row_windows3(k):
        return col3_ref[step_rows(k)] + col3_ref[step_rows(k, 1)] + col3_ref[step_rows(k, 2)]

    def mix3(k, carry):
        total, square = carry
        rows = step_rows(k)
        values = e_ref[rows]
        share = widen(inv3_ref[rows])
        pooled = row_windows3(k) * share - rounded(affine(values, factor3, shift3))
        pooled = jnp.where(share > 0.0, pooled, 0.0)
        mixed = values + scale3 * pooled
        pool3_ref[rows] = pooled
        mix3_ref[rows] = mixed
        return (total + fold(mixed), square + fold(mixed * mixed))

    total, square = sweep(mix3, (nothing3, nothing3))
    mean4, scaling4 = norm_terms(total, square, count_three)
    factor4 = scaling4 * gain4
    shift4 = bias4 - mean4 * scaling4 * gain4
    normal4 = (spread(scaling4, WIDE), spread(-mean4 * scaling4, WIDE))

    def prepare3(k, d_bias):
        rows = step_rows(k)
        h3_ref[rows] = affine(mix3_ref[rows], factor4, shift4).astype(bf16)
        goal = goal_ref[0, rows].astype(f32)
        goal = jnp.where(widen(inv3_ref[rows]) > 0.0, goal, 0.0)
        low_goal = (scale4 * goal).astype(bf16)
        dy3_ref[rows] = low_goal
        return d_bias + fold(low_goal.astype(f32))

    acc_three[7] += sweep(prepare3, nothing3)

    def keep(ref, value, place=slice(None)):
        if pairs == 1:
            ref[place] = value.astype(ref.dtype)
        else:

            @pl.when(pair == 0)
            def _():
                ref[place] = value

            @pl.when(pair > 0)
            def _():
                ref[place] += value

    def begin_chunk(at):
        lanes = slice(at, at + 256)
        hid3_ref[:, lanes] = product(h3_ref[...], w3_ref[:, lanes])
        dhid3_ref[:, lanes] = product_nt(dy3_ref[...], w4_ref[lanes])

    begin_chunk(0)
    for at in range(0, HID3, 256):
        if at + 256 < HID3:
            begin_chunk(at + 256)
        for lane in (at, at + 128):
            lanes = slice(lane, lane + 128)
            total = nothing
            for k in range(STEPS):
                rows = step_rows(k)
                active, slope = gelu_pair(hid3_ref[rows, lanes] + vec_hid_three_ref[:, lanes])
                u3_ref[rows, lanes] = active.astype(bf16)
                low = (slope * dhid3_ref[rows, lanes]).astype(bf16)
                g3_ref[rows, lanes] = low
                total = total + fold(low.astype(f32))
            acc_hid_three[:, lanes] += total
        lanes = slice(at, at + 256)
        out = product(u3_ref[:, lanes], w4_ref[lanes])
        d_low = product_nt(g3_ref[:, lanes], w3_ref[:, lanes])
        result_ref[0] = out if at == 0 else result_ref[0] + out
        dx3_ref[...] = d_low if at == 0 else dx3_ref[...] + d_low
        keep(gw3_ref, product_tn(h3_ref[...], g3_ref[:, lanes]), (slice(None), lanes))
        keep(gw4_ref, product_tn(u3_ref[:, lanes], dy3_ref[...]), lanes)

    def finish3(k, carry):
        d_scale, d_shift, d_gain = carry
        rows = step_rows(k)
        valid = widen(inv3_ref[rows]) > 0.0
        mixed = mix3_ref[rows]
        out = jnp.where(valid, result_ref[0, rows] + out_bias3, 0.0)
        result_ref[0, rows] = mixed + scale4 * out
        d_scale = d_scale + fold(out * goal_ref[0, rows].astype(f32))
        d_low = dx3_ref[rows]
        normal = affine(mixed, *normal4)
        return (d_scale, d_shift + fold(d_low), d_gain + fold(d_low * normal))

    d_scale, d_shift, d_gain = sweep(finish3, (nothing3, nothing3, nothing3))
    acc_three[6] += d_scale
    acc_three[5] += d_shift
    acc_three[4] += d_gain
    mean_shift = by_image(d_shift * gain4) / count_three
    mean_gain = by_image(d_gain * gain4) / count_three
    back_gain4 = scaling4 * gain4
    back_mean4 = spread(-scaling4 * mean_shift, WIDE)
    back_normal4 = spread(scaling4 * mean_gain, WIDE)

    def unmix3(k, d_scale):
        rows = step_rows(k)
        share = widen(inv3_ref[rows])
        valid = share > 0.0
        normal = affine(mix3_ref[rows], *normal4)
        back = affine(dx3_ref[rows], back_gain4, back_mean4) - scaled(normal, back_normal4)
        d_mixed = jnp.where(valid, back + goal_ref[0, rows].astype(f32), 0.0)
        dx3_ref[rows] = d_mixed
        d_scale = d_scale + fold(pool3_ref[rows] * d_mixed)
        weighted = scale3 * d_mixed * share
        col3_ref[step_rows(k, 1)] = weighted + from_left(weighted) + from_right(weighted)
        return d_scale

    acc_three[3] += sweep(unmix3, nothing3)
    normal3 = (spread(scaling3, WIDE), spread(-mean3 * scaling3, WIDE))

    def unpool3(k, carry):
        d_shift, d_gain = carry
        rows = step_rows(k)
        valid = widen(inv3_ref[rows]) > 0.0
        d_normal = jnp.where(valid, row_windows3(k) - scale3 * dx3_ref[rows], 0.0)
        pool3_ref[rows] = d_normal
        normal = affine(e_ref[rows], *normal3)
        return (d_shift + fold(d_normal), d_gain + fold(d_normal * normal))

    d_shift, d_gain = sweep(unpool3, (nothing3, nothing3))
    acc_three[2] += d_shift
    acc_three[1] += d_gain
    mean_shift = by_image(d_shift * gain3) / count_three
    mean_gain = by_image(d_gain * gain3) / count_three
    back_gain3 = scaling3 * gain3
    back_mean3 = spread(-scaling3 * mean_shift, WIDE)
    back_normal3 = spread(scaling3 * mean_gain, WIDE)

    def unnorm3(k, d_bias):
        rows = step_rows(k)
        valid = widen(inv3_ref[rows]) > 0.0
        normal = affine(e_ref[rows], *normal3)
        back = affine(pool3_ref[rows], back_gain3, back_mean3) - scaled(normal, back_normal3)
        low = jnp.where(valid, dx3_ref[rows] + back, 0.0).astype(bf16)
        dpre_ref[rows] = low
        return d_bias + fold(low.astype(f32))

    acc_three[0] += sweep(unnorm3, nothing3)
    keep(gwe_ref, product_tn(patch_ref[...], dpre_ref[...]))
    dpatch_ref[0:AREA] = product_nt(dpre_ref[...], we_ref[...])
    dpatch_ref[AREA : AREA + LINE] = jnp.zeros((LINE, 9 * C2), f32)

    def gather_back(k, carry):
        rows = step_rows(k)

        def tap(ky, kx, source):
            at = (3 * ky + kx) * C2
            value = dpatch_ref[source, at : at + C2]
            if ky != kx:
                at = (3 * kx + ky) * C2
                value = jnp.where(flipped, dpatch_ref[source, at : at + C2], value)
            return value

        sources = []
        for ky in range(3):
            source = step_rows(k, 1 if ky == 0 else 0)
            sources.append(
                (tap(ky, 1, source), tap(ky, 2, source) + from_right(tap(ky, 0, source)))
            )
        for pc in range(2):
            for pr, value in ((0, sources[1][pc]), (1, sources[2][pc] + sources[0][pc])):
                plane = pr * 2 + pc
                valid = inv_ref[plane, rows] > 0.0
                back_ref[plane, rows] = jnp.where(valid, rounded(value), 0.0)
        return carry

    sweep(gather_back, 0)

    if pairs == 1:
        pack_blocks(range(2, 5))

    normal2 = (spread(scaling2, C2), spread(-mean2 * scaling2, C2))

    def begin_back(plane):
        low_goal = (scale2 * back_ref[plane]).astype(bf16)
        dy_ref[plane_rows(plane)] = low_goal
        hid_ref[plane % 2] = product_nt(low_goal, w2_ref[...])
        return fold(low_goal.astype(f32))

    d_out_bias = begin_back(0)
    d_shift, d_gain = nothing, nothing
    sums = [nothing] * (HID2 // 128)
    new_gw1, new_gw2 = None, None
    for plane in range(4):
        if plane < 3:
            d_out_bias = d_out_bias + begin_back(plane + 1)
        for k in range(STEPS):
            rows = step_rows(k)
            part = slice(plane * AREA + k * STEP, plane * AREA + k * STEP + STEP)
            for n, at in enumerate(range(0, HID2, 128)):
                lanes = slice(at, at + 128)
                low = g_ref[part, lanes].astype(f32) * hid_ref[plane % 2, rows, lanes]
                low = low.astype(bf16)
                g_ref[part, lanes] = low
                sums[n] = sums[n] + fold(low.astype(f32))
        flat = plane_rows(plane)
        d_low = product_nt(g_ref[flat], w1_ref[...])
        dx_ref[plane] = d_low
        d_shift = d_shift + fold(d_low)
        d_gain = d_gain + fold(d_low * affine(mix_ref[plane], *normal2))
        part_gw1 = product_tn(h_ref[flat], g_ref[flat])
        part_gw2 = product_tn(dy_ref[flat], u_ref[flat])
        new_gw1 = part_gw1 if plane == 0 else new_gw1 + part_gw1
        new_gw2 = part_gw2 if plane == 0 else new_gw2 + part_gw2
    new_gw2 = new_gw2.T
    for n, value in enumerate(sums):
        acc_hid_two[:, n * 128 : n * 128 + 128] += value
    acc_two[6] += d_out_bias
    acc_two[4] += d_shift
    acc_two[3] += d_gain
    mean_out[0, 0] = spread(by_image(d_shift * gain2) / count_two, 128)
    mean_out[0, 1] = spread(by_image(d_gain * gain2) / count_two, 128)
    keep(gw1_ref, new_gw1)
    keep(gw2_ref, new_gw2)
    d_scale = fold(w2_ref[...].astype(f32) * new_gw2) + out_bias * d_out_bias
    acc_two[5] += d_scale / scale2

    def finish():
        if pairs > 1:
            pack_blocks(range(5))
        else:
            pack_blocks(range(2))

        def filler(number, carry):
            put_block(number, jnp.zeros((HALF, 128), bf16))
            return carry

        lax.fori_loop(USED, slots, filler, 0)

        flat_ref[...] = jnp.zeros(flat_ref.shape, f32)

        def put(at, total, length):
            if at % 128:
                room = jnp.zeros((8, 128), f32)
                if total.shape[1] < length + BS:
                    total = jnp.concatenate([total, room], axis=1)
                total = pltpu.roll(total, BS, 1)
            whole = jnp.sum(total, axis=0, keepdims=True)
            done = -(at % 128)
            row = at // 128
            lane = 0
            while done < length:
                first = max(0, -done)
                last = min(128, length - done)
                flat_ref[row : row + 1, first:last] = whole[:, lane + first : lane + last]
                done += 128
                lane += 128
                row += 1

        at = 3 * C2
        for n in range(3, 6):
            put(at, acc_two[n], C2)
            at += C2
        put(at, acc_hid_two[...], HID2)
        at += HID2
        put(at, acc_two[6], C2)
        at += C2
        for n in range(7):
            put(at, acc_three[n], C3)
            at += C3
        put(at, acc_hid_three[...], HID3)
        at += HID3
        put(at, acc_three[7], C3)

    at_pair(pairs - 1, finish)


def run_main(places, sizes, state, goal, vectors, weights, strip_count):
    pairs = goal.shape[0]
    slots = places[0].shape[0]
    half = slots // 2 + 1
    if pairs == 1:
        state = held_in(pltpu.VMEM, *state)
    weights = held_in(pltpu.VMEM, *weights)
    _, inv, _, mix, stat = state
    state_shapes = [STATE[1], STATE[3], STATE[4]]
    grad_kind = bf16 if pairs == 1 else f32
    wide_f32 = pltpu.VMEM((AREA, WIDE), f32)
    wide_bf16 = pltpu.VMEM((AREA, WIDE), bf16)
    scratch = [
        pltpu.VMEM((4, AREA + LINE, C2), f32),
        pltpu.VMEM((2, AREA, HID2), f32),
        pltpu.VMEM((4 * AREA, HID2), bf16),
        pltpu.VMEM((4 * AREA, HID2), bf16),
        pltpu.VMEM((4 * AREA, C2), bf16),
        pltpu.VMEM((4 * AREA, C2), bf16),
        pltpu.VMEM((AREA, 9 * C2), bf16),
        pltpu.VMEM((AREA + LINE, 9 * C2), f32),
        pltpu.VMEM((AREA, 128), f32),
        wide_f32,
        pltpu.VMEM((AREA + 2 * LINE, WIDE), f32),
        wide_f32,
        wide_f32,
        wide_f32,
        pltpu.VMEM((AREA, HID3), f32),
        pltpu.VMEM((AREA, HID3), f32),
        pltpu.VMEM((AREA, HID3), bf16),
        pltpu.VMEM((AREA, HID3), bf16),
        wide_bf16,
        wide_bf16,
        wide_bf16,
        pltpu.VMEM((C2, HID2), grad_kind),
        pltpu.VMEM((HID2, C2), grad_kind),
        pltpu.VMEM((9 * C2, WIDE), grad_kind),
        pltpu.VMEM((WIDE, HID3), grad_kind),
        pltpu.VMEM((HID3, WIDE), grad_kind),
        pltpu.VMEM((7, 8, C2), f32),
        pltpu.VMEM((8, HID2), f32),
        pltpu.VMEM((8, 8, WIDE), f32),
        pltpu.VMEM((8, HID3), f32),
    ]
    out_shapes = [(half, HALF, 128), (half, HALF, 128), (VEC_BLOCKS * HALF, 128)]
    make = pltpu.VMEM if pairs == 1 else jax.ShapeDtypeStruct
    return pl.pallas_call(
        functools.partial(main_kernel, pairs, strip_count, slots),
        grid=() if pairs == 1 else (pairs,),
        in_specs=[SMEM] * 3
        + pair_specs(pairs, state_shapes + [goal.shape[1:]], pl.Buffered(1))
        + whole_specs(pairs, [vector.shape for vector in vectors])
        + [VMEM_BLOCK] * 5,
        out_specs=pair_specs(pairs, [(AREA, WIDE)] + BACK) + whole_specs(pairs, out_shapes),
        out_shape=pair_arrays(pairs, [(AREA, WIDE)] + BACK, [f32] * 4)
        + [make(shape, kind) for shape, kind in zip(out_shapes, (bf16, bf16, f32))],
        scratch_shapes=scratch,
        compiler_params=pltpu.CompilerParams(
            vmem_limit_bytes=(40 if pairs == 1 else 56) * 1024 * 1024,
            fuse_transposed_lhs_in_matmul=True,
        ),
        name="blocks",
    )(*places, sizes, inv, mix, stat, goal, *vectors, *weights)


def exit_kernel(
    pairs,
    strip_count,
    size_ref,
    x_in,
    inv_in,
    pool_in,
    mix_in,
    stat_in,
    zed_in,
    dx_in,
    mean_in,
    flat_ref,
    vec_two_ref,
    payload_hbm,
    vector_ref,
    payload_ref,
    image_ref,
    col_ref,
    dx_ref,
    back_ref,
    acc_ref,
    sem,
):
    pair = pl.program_id(0) if pairs > 1 else 0
    x_ref, inv_ref, pool_ref, mix_ref, stat_ref, zed_ref, low_ref, mean_ref = (
        ref.at[0] for ref in (x_in, inv_in, pool_in, mix_in, stat_in, zed_in, dx_in, mean_in)
    )
    shape = Geometry(size_ref, pair)
    count_two = shape.count_two
    gain1, bias1, scale1, gain2 = (vec_two_ref[n : n + 1] for n in range(4))
    mean1, scaling1, mean2, scaling2 = (stat_ref[n] for n in range(4))
    normal2 = (scaling2, -mean2 * scaling2)
    clear_edges(col_ref)
    nothing = jnp.zeros((8, C2), f32)
    back_gain2 = scaling2 * gain2
    back_mean2 = -scaling2 * mean_ref[0]
    back_normal2 = scaling2 * mean_ref[1]

    if pairs > 1:

        @pl.when(pair == 0)
        def _():
            acc_ref[...] = jnp.zeros(acc_ref.shape, f32)

    def add_up(n, total):
        acc_ref[n] = total if pairs == 1 else acc_ref[n] + total

    def unmix(k, d_scale):
        rows = step_rows(k)
        for pr in range(2):
            weighted = []
            for pc in range(2):
                plane = pr * 2 + pc
                share = inv_ref[plane, rows]
                normal = affine(mix_ref[plane, rows], *normal2)
                back = affine(low_ref[plane, rows], back_gain2, back_mean2)
                back = back - scaled(normal, back_normal2)
                d_mixed = jnp.where(share > 0.0, zed_ref[plane, rows] + back, 0.0)
                dx_ref[plane, rows] = d_mixed
                d_scale = d_scale + fold(pool_ref[plane, rows] * d_mixed)
                weighted.append(scale1 * d_mixed * share)
            put_col_windows(col_ref, pr, k, *weighted)
        return d_scale

    add_up(2, sweep(unmix, nothing))
    normal1 = (spread(scaling1, C2), spread(-mean1 * scaling1, C2))

    def unpool(k, carry):
        d_shift, d_gain = carry
        rows = step_rows(k)
        for pc in range(2):
            windows = row_windows(col_ref, pc, k)
            for pr in range(2):
                plane = pr * 2 + pc
                valid = inv_ref[plane, rows] > 0.0
                d_normal = windows[pr] - scale1 * dx_ref[plane, rows]
                d_normal = jnp.where(valid, d_normal, 0.0)
                back_ref[plane, rows] = d_normal
                normal = affine(x_ref[plane, rows], *normal1)
                d_shift = d_shift + fold(d_normal)
                d_gain = d_gain + fold(d_normal * normal)
        return (d_shift, d_gain)

    d_shift, d_gain = sweep(unpool, (nothing, nothing))
    add_up(1, d_shift)
    add_up(0, d_gain)
    mean_shift = by_image(d_shift * gain1) / count_two
    mean_gain = by_image(d_gain * gain1) / count_two
    back_gain1 = scaling1 * gain1
    back_mean1 = spread(-scaling1 * mean_shift, C2)
    back_normal1 = spread(scaling1 * mean_gain, C2)

    def unnorm(k, carry):
        rows = step_rows(k)
        for plane in range(4):
            normal = affine(x_ref[plane, rows], *normal1)
            back = affine(back_ref[plane, rows], back_gain1, back_mean1)
            back = back - scaled(normal, back_normal1)
            valid = inv_ref[plane, rows] > 0.0
            dx_ref[plane, rows] = jnp.where(valid, dx_ref[plane, rows] + back, 0.0)
        return carry

    sweep(unnorm, 0)

    def give_back(plane, here, spot, there):
        image_ref[spot, there] = dx_ref[plane, here]

    image_ref[...] = jnp.zeros(image_ref.shape, f32)
    each_image(size_ref, pair, give_back)

    for spot in range(2 * STRIPS):
        target = strip_place(pair, spot, strip_count)
        for within in range(SR):
            rows = slice(within * CW, within * CW + CW)
            payload_ref[target, within] = image_ref[spot, rows].astype(bf16)

    def finish():
        copy = pltpu.make_async_copy(payload_ref, payload_hbm, sem)
        copy.start()
        vector_ref[...] = flat_ref[...]
        for n in range(3):
            vector_ref[n : n + 1] = jnp.sum(acc_ref[n], axis=0, keepdims=True)
        copy.wait()

    if pairs == 1:
        finish()
    else:
        pl.when(pair == pairs - 1)(finish)


def run_exit(sizes, state, back, flat, vec_two, strip_count):
    pairs = strip_count // 8
    payload = (strip_count, SR, CW, C2)
    make = pltpu.VMEM if pairs == 1 else jax.ShapeDtypeStruct
    plane_f32 = pltpu.VMEM((4, AREA, C2), f32)
    arrays = [*state, *back]
    if pairs == 1:
        arrays = held_in(pltpu.VMEM, *arrays)
    return pl.pallas_call(
        functools.partial(exit_kernel, pairs, strip_count),
        grid=() if pairs == 1 else (pairs,),
        in_specs=[SMEM]
        + pair_specs(pairs, STATE + BACK, pl.Buffered(1))
        + whole_specs(pairs, [flat.shape, vec_two.shape]),
        out_specs=[HBM] + whole_specs(pairs, [flat.shape]),
        out_shape=[pltpu.HBM(payload, bf16), make(flat.shape, f32)],
        scratch_shapes=[
            pltpu.VMEM(payload, bf16),
            pltpu.VMEM((2 * STRIPS, STRIP_ROWS, C2), f32),
            pltpu.VMEM((4, AREA + 2 * LINE, C2), f32),
            plane_f32,
            plane_f32,
            pltpu.VMEM((3, 8, C2), f32),
            pltpu.SemaphoreType.DMA,
        ],
        compiler_params=roomy(8 if pairs == 1 else 40),
        name="exit",
    )(sizes, *arrays, flat, vec_two)


def dense_blocks(values):
    return jnp.concatenate([values[:, :HALF], values[:, HALF:]], axis=2).astype(bf16)


def pack_kernel(master_ref, dense_ref):
    dense_ref[...] = dense_blocks(master_ref[...])


def pack(master):
    owned = master.shape[0]
    return pl.pallas_call(
        pack_kernel,
        out_shape=jax.ShapeDtypeStruct((owned, HALF, 2 * BS), bf16),
        name="pack",
    )(master)


def pack_pieces_kernel(place_ref, master_ref, pixel_ref, *refs):
    out_refs, wide_ref = refs[:-1], refs[-1]
    owned = master_ref.shape[0]
    slots = pixel_ref.shape[2]

    def widen_row(row, carry):
        start = pl.multiple_of(row * CW * slots, 8)
        values = pixel_ref[row].astype(f32).reshape(CW * slots, C2)
        wide_ref[pl.ds(start, CW * slots)] = values
        return carry

    lax.fori_loop(0, SR, widen_row, 0)
    dense = dense_blocks(master_ref[...]).reshape(owned * HALF, 2 * BS)
    for k, ref in enumerate(out_refs):
        ref[STRIP_ROWS : STRIP_ROWS + owned * HALF] = dense
        for other in range(2):
            slot = place_ref[0] ^ (2 * k + other)
            first = other * (STRIP_ROWS + owned * HALF)
            strip = wide_ref[pl.ds(slot, STRIP_ROWS, stride=slots)]
            ref[first : first + STRIP_ROWS] = strip.astype(bf16)


def pack_pieces(place, master, pixels):
    slots = pixels.shape[2]
    shape = (master.shape[0] * HALF + 2 * STRIP_ROWS, 2 * BS)
    return pl.pallas_call(
        pack_pieces_kernel,
        in_specs=[SMEM] + [VMEM_BLOCK] * 2,
        out_specs=[VMEM_BLOCK] * (slots // 2),
        out_shape=[pltpu.VMEM(shape, bf16)] * (slots // 2),
        scratch_shapes=[pltpu.VMEM((STRIP_ROWS * slots, C2), f32)],
        compiler_params=roomy(8),
        name="pack",
    )(place, master, pixels)


def fold_pair_kernel(near_ref, got_ref, own_ref, *part_refs):
    share = own_ref.shape[0]

    def one(n, carry):
        for k in range(len(part_refs) + 1):
            total = near_ref[k * share + n].astype(f32) + got_ref[k * share + n].astype(f32)
            if k == 0:
                own_ref[n] = total
            else:
                part_refs[k - 1][n] = total.astype(bf16)
        return carry

    lax.fori_loop(0, share, one, 0, unroll=4)


def fold_pair(near, got, groups):
    shape = ((near.shape[0] - 1) // groups,) + near.shape[1:]
    return pl.pallas_call(
        fold_pair_kernel,
        in_specs=[VMEM_BLOCK] * 2,
        out_specs=[VMEM_BLOCK] * groups,
        out_shape=[pltpu.VMEM(shape, f32)] + [pltpu.VMEM(shape, bf16)] * (groups - 1),
        compiler_params=roomy(4),
        name="fold_pair",
    )(*held_in(pltpu.VMEM, near, got))


def fold_tile_kernel(pieces, spot_ref, *refs):
    piece_refs, refs = refs[:pieces], refs[pieces:]
    vector_refs, refs = refs[:pieces], refs[pieces:]
    out_refs, sum_ref = refs[:-1], refs[-1]
    groups = len(out_refs)
    share = out_refs[0].shape[0]
    owned = piece_refs[0].shape[0]
    total = vector_refs[0][...]
    for ref in vector_refs[1:]:
        total = total + ref[...]
    for n in range(sum_ref.shape[0]):
        sum_ref[n] = jnp.zeros((HALF, 128), f32)
    for n in range(VEC_BLOCKS):
        sum_ref[n] = total[n * HALF : (n + 1) * HALF]

    def one(n, carry):
        for k, out_ref in enumerate(out_refs):
            number = lax.rem(spot_ref[0] + k, groups) * share + n
            block = jnp.minimum(number, owned - 1)
            total = piece_refs[0][block].astype(f32)
            for ref in piece_refs[1:]:
                total = total + ref[block].astype(f32)
            rest = sum_ref[jnp.maximum(number - owned, 0)]
            out_ref[n] = jnp.where(number < owned, total, rest).astype(out_ref.dtype)
        return carry

    lax.fori_loop(0, share, one, 0, unroll=share <= 16)


def fold_tile(spot, pieces, vectors, extra, groups):
    shape = ((pieces[0].shape[0] + extra) // groups,) + pieces[0].shape[1:]
    return pl.pallas_call(
        functools.partial(fold_tile_kernel, len(pieces)),
        in_specs=[SMEM] + [VMEM_BLOCK] * (len(pieces) + len(vectors)),
        out_specs=[VMEM_BLOCK] * groups,
        out_shape=[pltpu.VMEM(shape, f32)] + [pltpu.VMEM(shape, bf16)] * (groups - 1),
        scratch_shapes=[pltpu.VMEM((extra, HALF, 128), f32)],
        compiler_params=roomy(8),
        name="fold_tile",
    )(spot, *held_in(pltpu.VMEM, *pieces, *vectors))


def fold_batch_kernel(owned, vector_weight, spot_ref, *refs):
    part_refs, (total_ref, norm_ref) = refs[:-2], refs[-2:]
    share = total_ref.shape[0]
    square = jnp.zeros((8, 128), f32)
    for n in range(share):
        total = part_refs[0][n].astype(f32)
        for ref in part_refs[1:]:
            total = total + ref[n].astype(f32)
        total_ref[n] = total.astype(bf16)
        weight = jnp.where(spot_ref[0] * share + n < owned, 1.0, vector_weight)
        square = square + weight * fold(total * total)
    square = jnp.sum(jnp.sum(square, axis=1, keepdims=True), axis=0, keepdims=True)
    norm_ref[...] = jnp.broadcast_to(square[None], norm_ref.shape)


def fold_batch(spot, parts, owned, tile_count):
    count = tile_count * len(parts)
    return pl.pallas_call(
        functools.partial(fold_batch_kernel, owned, 1.0 / tile_count),
        in_specs=[SMEM] + [VMEM_BLOCK] * len(parts),
        out_specs=[VMEM_BLOCK] * 2,
        out_shape=[pltpu.VMEM(parts[0].shape, bf16), pltpu.VMEM((count, 1, 128), f32)],
        name="fold_batch",
    )(spot, *held_in(pltpu.VMEM, *parts))


def update_kernel(owned, groups, spot_ref, norm_ref, *refs):
    quarters, refs = refs[:groups], refs[groups:]
    stat_hbm, out_hbm, (vector_ref, clip_ref), refs = refs[:5], refs[5:10], refs[10:12], refs[12:]
    stat_refs, out_refs, (in_sem, out_sem) = refs[:5], refs[5:10], refs[10:]
    master_ref, left_stat_ref, right_stat_ref, left_root_ref, right_root_ref = stat_refs
    grad_ref, left_ref, right_ref, new_ref, copy_ref = out_refs
    share = quarters[0].shape[0]
    spans = spans_of(owned)

    def copies_of(sources, targets, sems):
        return [
            [
                pltpu.make_async_copy(
                    source.at[pl.ds(*span)], target.at[pl.ds(*span)], sems.at[5 * n + k]
                )
                for k, (source, target) in enumerate(zip(sources, targets))
            ]
            for n, span in enumerate(spans)
        ]

    copies_in = copies_of(stat_hbm, stat_refs, in_sem)
    copies_out = copies_of(out_refs, out_hbm, out_sem)
    for copies in copies_in:
        for copy in copies:
            copy.start()
    norm = jnp.sqrt(jnp.sum(norm_ref[...], axis=0))
    factor = jnp.minimum(1.0, clip_limit / norm)
    left_half = lax.broadcasted_iota(jnp.int32, (HALF, 128), 1) < BS

    def summed(number):
        source = number // share
        local = number - source * share
        turn = lax.rem(spot_ref[0] - source + groups, groups)
        value = quarters[0][local].astype(f32)
        for k in range(1, groups):
            value = jnp.where(turn == k, quarters[k][local].astype(f32), value)
        return value * factor

    def side_by_side(first, count):
        sides = []
        for n in range(first, first + count, 2):
            dense = summed(n)
            turned = pltpu.roll(dense, BS, 1)
            if n + 1 < first + count:
                second = summed(n + 1)
                top = jnp.where(left_half, dense, pltpu.roll(second, BS, 1))
                low = jnp.where(left_half, turned, second)
                side = jnp.concatenate([top, low], axis=0)
                grad_ref[n + 1] = pltpu.roll(side, BS, 1)[:, :BS]
            else:
                side = jnp.concatenate([dense, turned], axis=0)[:, :BS]
            grad_ref[n] = side[:, :BS]
            sides.append(side.astype(bf16))
        return jnp.concatenate(sides, axis=1)

    def diagonal_of(count):
        order = (count * BS, count * BS)
        return lax.broadcasted_iota(jnp.int32, order, 0) // BS == (
            lax.broadcasted_iota(jnp.int32, order, 1) // BS
        )

    clip_ref[...] = norm
    for n in range(vector_ref.shape[0]):
        vector_ref[n] = summed(owned + n)
    for (first, length), arriving, leaving in zip(spans, copies_in, copies_out):
        parts = [(n, min(4, first + length - n)) for n in range(first, first + length, 4)]
        wides = [side_by_side(*part) for part in parts]
        tall = [
            jnp.where(diagonal_of(count), jnp.concatenate([wide] * count, axis=0), 0.0)
            for (_, count), wide in zip(parts, wides)
        ]
        lefts = [product_nt(one, wide) for one, wide in zip(tall, wides)]
        rights = [product_tn(wide, wide) for wide in wides]
        for copy in arriving:
            copy.wait()
        stepped = []
        for (start, count), wide in zip(parts, wides):
            roots = left_root_ref[pl.ds(start, count)].reshape(count * BS, BS).astype(bf16)
            stepped.append(product(roots, wide))
        for (start, count), left, right in zip(parts, lefts, rights):
            here = pl.ds(start, count)
            left_ref[here] = 0.5 * left_stat_ref[here] + 0.5 * left.reshape(count, BS, BS)
            for n in range(count):
                at = n // 2 * 128
                block = right[n * BS : n * BS + BS, at : min(at + 128, count * BS)]
                if n % 2:
                    block = pltpu.roll(block, BS, 1)
                right_ref[start + n] = 0.5 * right_stat_ref[start + n] + 0.5 * block[:, :BS]
        for (start, count), value in zip(parts, stepped):
            here = pl.ds(start, count)
            value = jnp.where(diagonal_of(count), value, 0.0).astype(bf16)
            roots = right_root_ref[here].reshape(count * BS, BS).astype(bf16)
            value = product(value, roots).reshape(count, BS, BS)
            new = master_ref[here] - rate_matrix * value
            new_ref[here] = new
            copy_ref[here] = new.astype(bf16)
        for copy in leaving:
            copy.start()
    for leaving in copies_out:
        for copy in leaving:
            copy.wait()


def spans_of(owned):
    spans = []
    first = 0
    while first < owned:
        length = min(8 if first == 0 else 12, owned - first)
        spans.append((first, length))
        first += length
    return spans


def update(spot, norm, quarters, extra, *stats):
    shape = stats[0].shape
    groups = len(quarters)
    types = [f32] * 4 + [bf16]
    steps = len(spans_of(shape[0]))
    return pl.pallas_call(
        functools.partial(update_kernel, shape[0], groups),
        in_specs=[SMEM] + [VMEM_BLOCK] * (groups + 1) + [HBM] * 5,
        out_specs=[HBM] * 5 + [VMEM_BLOCK] * 2,
        out_shape=[pltpu.HBM(shape, kind) for kind in types]
        + [
            pltpu.VMEM((extra, HALF, 128), f32),
            pltpu.VMEM((1, 128), f32),
        ],
        scratch_shapes=[pltpu.VMEM(shape, f32)] * 5
        + [pltpu.VMEM(shape, kind) for kind in types]
        + [
            pltpu.SemaphoreType.DMA((5 * steps,)),
            pltpu.SemaphoreType.DMA((5 * steps,)),
        ],
        compiler_params=roomy(20),
        name="update",
    )(spot, *held_in(pltpu.VMEM, norm, *quarters), *held_in(pltpu.HBM, *stats))


def share_out(pieces, axis):
    return lax.all_to_all(pieces, axis, split_axis=0, concat_axis=0, tiled=True)


def swap(piece, distance):
    count = lax.axis_size("tile")
    return lax.ppermute(piece, "tile", [(i, i ^ distance) for i in range(count)])


def on_device(
    pixels,
    buckets,
    slot_owner_table,
    out_grad,
    master,
    left_stat,
    right_stat,
    left_root,
    right_root,
    vectors,
    moment,
):
    tile_count = lax.axis_size("tile")
    tile_place = lax.axis_index("tile")
    slot_count = pixels.shape[2]
    group_count = tile_count // STRIPS
    pairs = group_count // 2
    owned = master.shape[0]
    slots = owned * tile_count
    batch_count = lax.axis_size("batch")
    spot = lax.axis_index("batch").astype(jnp.int32).reshape(1)
    extra = extra_of(owned, batch_count)
    place = tile_place.astype(jnp.int32).reshape(1)
    paired = tile_count == 8
    if paired:
        mine = pack_pieces(place, master, pixels[0, 0].transpose(1, 2, 0, 3))
        mine = [mine[0]] + [swap(mine[k], 2 * k) for k in range(1, tile_count // 2)]
        pieces = strips = mine + [swap(piece, 1) for piece in mine]
    else:
        pieces = [lax.all_gather(pack(master), "tile", axis=0, tiled=True).reshape(-1, 2 * BS)]
        strips = share_out(pixels.reshape(tile_count, STRIP, C2), "tile")
        strips = [jnp.pad(strips, ((0, 0), (0, STRIP_ROWS - STRIP), (0, 0)))]

    numbers = jnp.arange(slots, dtype=jnp.int32)
    slot_of = jnp.sum(
        jnp.where(slot_owner_table[None, :] == numbers[:, None], numbers[None, :], 0), axis=1
    )
    owner = slot_of // owned
    within = slot_of - owner * owned
    place_of = slot_of
    if paired:
        apart = owner ^ tile_place
        apart = (apart & 1) * (tile_count // 2) + (apart >> 1)
        slot_of = place_of = within + owned * apart
    half = slots // 2
    near_place = jnp.where(place_of < half, place_of, half)
    far_place = jnp.where(place_of < half, half, place_of - half)
    image_ids = lax.dynamic_index_in_dim(
        buckets.reshape(group_count, slot_count), tile_place, 1, keepdims=False
    )
    turned = image_ids >= 2
    heights = jnp.where(image_ids == 0, 5 * CH // 9, jnp.where(image_ids == 1, 7 * CH // 9, CH))
    breadths = jnp.where(image_ids == 0, CW, jnp.where(image_ids == 1, 7 * CW // 9, 5 * CW // 9))
    sizes = jnp.stack(
        [
            jnp.where(turned, breadths, heights),
            jnp.where(turned, heights, breadths),
            turned,
        ],
        axis=1,
    )
    sizes = sizes.reshape(-1).astype(jnp.int32)

    two = 6 * C2 + HID2 + C2
    vec_two = jnp.concatenate([vectors[: 6 * C2], vectors[6 * C2 + HID2 : two]]).reshape(7, C2)
    vec_hid_two = vectors[6 * C2 : 6 * C2 + HID2].reshape(1, HID2)
    wide_end = two + 7 * C3
    vec_three = jnp.concatenate([vectors[two:wide_end], vectors[wide_end + HID3 :]])
    vec_three = jnp.pad(vec_three.reshape(8, C3), ((0, 0), (0, WIDE - C3)))
    vec_hid_three = vectors[wide_end : wide_end + HID3].reshape(1, HID3)

    flips = turned.reshape(-1, 1, 1, 1)
    goal = out_grad.reshape(2 * pairs, H3, W3, C3)
    goal = jnp.where(flips, goal.transpose(0, 2, 1, 3), goal)[:, :LINES]
    goal = goal.reshape(pairs, 2, LINES, W3, C3).transpose(0, 2, 3, 1, 4)
    goal = goal.reshape(pairs, LINES, 2 * W3, C3)
    goal = jnp.pad(goal, ((0, 0), (0, 0), (0, LINE - 2 * W3), (0, WIDE - C3)))
    goal = goal.reshape(pairs, AREA, WIDE)

    weights = run_unpack(slot_of, pieces)
    state = run_entry(place, sizes, strips, vec_two, tile_count)
    result, *back, near, far, flat = run_main(
        (near_place, far_place),
        sizes,
        state,
        goal,
        (vec_two, vec_hid_two, vec_three, vec_hid_three),
        weights,
        tile_count,
    )
    pixel_back, vector = run_exit(sizes, state, back, flat, vec_two, tile_count)
    if paired:
        own, *parts = fold_pair(near, swap(far, 1), tile_count // 2)
        pieces = [own] + [swap(part, 2 * k + 2) for k, part in enumerate(parts)]
        vector, _ = lax.optimization_barrier((vector, parts[0]))
        vector = vector + swap(vector, 1)
        vectors_in = [vector] + [swap(vector, 2 * k) for k in range(1, tile_count // 2)]
    else:
        outgoing = jnp.concatenate([near[:half], far[:half]], axis=0)
        pieces = list(share_out(outgoing.reshape(tile_count, owned, HALF, 128), "tile"))
        vectors_in = list(lax.all_gather(vector, "tile"))
    result, pieces[1] = lax.optimization_barrier((result, pieces[1]))
    result = result.reshape(pairs, LINES, LINE, WIDE)[:, :, : 2 * W3, :C3]
    result = result.reshape(pairs, LINES, W3, 2, C3).transpose(0, 3, 1, 2, 4)
    result = result.reshape(2 * pairs, LINES, W3, C3)
    result = jnp.pad(result, ((0, 0), (0, H3 - LINES), (0, 0), (0, 0)))
    result = jnp.where(flips, result.transpose(0, 2, 1, 3), result)
    result = result.reshape(out_grad.shape)
    result = with_layout_constraint(result, Layout(major_to_minor=(0, 1, 2, 4, 5, 3, 6)))
    result, vectors_in[0] = lax.optimization_barrier((result, vectors_in[0]))
    own, *parts = fold_tile(spot, pieces, vectors_in, extra, batch_count)
    pixel_back, parts[0] = lax.optimization_barrier((pixel_back, parts[0]))
    returned = share_out(pixel_back, "tile")
    parts = [
        lax.ppermute(part, "batch", [(i, (i + k + 1) % batch_count) for i in range(batch_count)])
        for k, part in enumerate(parts)
    ]
    quarter, norm = fold_batch(spot, [own] + parts, owned, tile_count)
    returned, norm = lax.optimization_barrier((returned, norm))
    norm = share_out(norm, ("batch", "tile"))
    returned = returned.astype(f32).reshape(pixels.shape)
    returned = with_layout_constraint(returned, Layout(major_to_minor=(0, 1, 3, 4, 2, 5)))
    returned, quarter = lax.optimization_barrier((returned, quarter))
    quarters = [quarter] + [
        lax.ppermute(quarter, "batch", [(i, (i + k) % batch_count) for i in range(batch_count)])
        for k in range(1, batch_count)
    ]
    block_grad, left_new, right_new, master_new, weight_copy, whole_vector, clip = update(
        spot, norm, quarters, extra, master, left_stat, right_stat, left_root, right_root
    )
    clip_norm = clip[0, 0]
    share = vectors.shape[0] // tile_count
    whole_vector = whole_vector.reshape(-1)
    vec_grad = lax.dynamic_slice_in_dim(whole_vector, tile_place * share, share, 0)
    vec_moment = moment + vec_grad * vec_grad
    own_vectors = lax.dynamic_slice_in_dim(vectors, tile_place * share, share, 0)
    vec_new = own_vectors - rate_vector * vec_grad / (jnp.sqrt(vec_moment) + eps_adagrad)
    return (
        result,
        returned,
        clip_norm,
        block_grad,
        left_new,
        right_new,
        master_new,
        weight_copy,
        vec_grad,
        vec_moment,
        vec_new,
    )


def solution(mesh):
    placed = (
        P("batch", "tile", None, None, None, None),
        P("batch"),
        P(),
        P("batch", "tile", None, None, None, None, None),
        P("tile", None, None),
        P("tile", None, None),
        P("tile", None, None),
        P("tile", None, None),
        P("tile", None, None),
        P(),
        P("tile"),
    )
    return jax.shard_map(
        on_device,
        mesh=mesh,
        in_specs=placed,
        out_specs=(
            P("batch", "tile", None, None, None, None, None),
            P("batch", "tile", None, None, None, None),
            P(),
            P("tile", None, None),
            P("tile", None, None),
            P("tile", None, None),
            P("tile", None, None),
            P("tile", None, None),
            P("tile"),
            P("tile"),
            P("tile"),
        ),
        check_vma=False,
    )
```

```python
import functools

import jax
import jax.numpy as jnp
from jax import lax
from jax.experimental import pallas as pl
from jax.experimental.layout import Layout, with_layout_constraint
from jax.experimental.pallas import tpu as pltpu
from jax.sharding import PartitionSpec as P

C2 = 128
HID2 = 512
C3 = 320
HID3 = 1280
CH = 36
CW = 36
STRIPS = 4
BS = 64
SR = CH // STRIPS
H3 = CH // 2
W3 = CW // 2
LONG = 7 * CH // 9
LINES = LONG // 2
WIDE = 384
LINE = 40
AREA = LINES * LINE
STEP = 2 * LINE
STEPS = AREA // STEP
HALF = BS // 2
STRIP = SR * CW
STRIP_ROWS = STRIP + -STRIP % 16

eps_norm = 1e-05
clip_limit = 1.0
rate_matrix = 0.3
rate_vector = 0.3
eps_adagrad = 1e-08
f32 = jnp.float32
bf16 = jnp.bfloat16

SHAPES = [(C2, HID2), (HID2, C2), (9 * C2, C3), (C3, HID3), (HID3, C3)]
USED = sum(rows // BS * (cols // BS) for rows, cols in SHAPES)
VEC_ROWS = (6 * C2 + HID2 + C2 + C3 + 6 * C3 + HID3 + C3) // 128


VEC_BLOCKS = -(-VEC_ROWS // HALF)


def extra_of(owned, groups):
    return VEC_BLOCKS + -(owned + VEC_BLOCKS) % groups


def product(left, right):
    return jnp.dot(left, right, preferred_element_type=f32)


def product_nt(left, right):
    return lax.dot_general(left, right, (((1,), (1,)), ((), ())), preferred_element_type=f32)


def product_tn(left, right):
    return lax.dot_general(left, right, (((0,), (0,)), ((), ())), preferred_element_type=f32)


def gelu_pair(values):
    bell = jnp.exp2(values * values * (-0.5 * 1.4426950408889634))
    step = pl.reciprocal(1.0 + (0.3275911 * 0.7071067811865476) * jnp.abs(values), approx=True)
    tail = step * (
        0.5 * 0.254829592
        + step
        * (
            0.5 * -0.284496736
            + step
            * (0.5 * 1.421413741 + step * (0.5 * -1.453152027 + step * (0.5 * 1.061405429)))
        )
    )
    tail = tail * bell
    share = jnp.where(values >= 0.0, 1.0 - tail, tail)
    return (values * share, share + values * (bell * 0.3989422804014327))


def fold(values):
    chans = values.shape[-1]
    return jnp.sum(values.reshape(-1, 8, chans), axis=0)


def by_image(total):
    total = total + pltpu.roll(total, 4, 0)
    total = total + pltpu.roll(total, 2, 0)
    return jnp.sum(total, axis=1, keepdims=True)


def line(pattern):
    return jnp.concatenate([pattern] * (LINE // 8), axis=0)


def spread(pattern, chans):
    return jnp.broadcast_to(pattern, (8, chans))


def affine(values, factor, shift):
    tiles = values.reshape(-1, 8, values.shape[-1])
    return (tiles * factor + shift).reshape(values.shape)


def scaled(values, factor):
    tiles = values.reshape(-1, 8, values.shape[-1])
    return (tiles * factor).reshape(values.shape)


def from_left(values):
    return pltpu.roll(values, 2, 0)


def from_right(values):
    return pltpu.roll(values, values.shape[0] - 2, 0)


def rounded(values):
    return values.astype(bf16).astype(f32)


def widen(values):
    return jnp.concatenate([values] * (WIDE // 128), axis=-1)


def norm_terms(total, square, count):
    mean = by_image(total) / count
    scaling = lax.rsqrt(by_image(square) / count - mean * mean + eps_norm)
    return (mean, scaling)


def sweep(visit, start):
    return lax.fori_loop(0, STEPS, visit, start, unroll=True)


def step_rows(k, lines=0):
    start = k * STEP + lines * LINE
    return pl.ds(start if isinstance(k, int) else pl.multiple_of(start, LINE), STEP)


def held_in(space, *arrays):
    return [pltpu.with_memory_space_constraint(array, space) for array in arrays]


VMEM_BLOCK = pl.BlockSpec(memory_space=pltpu.VMEM)
HBM = pl.BlockSpec(memory_space=pltpu.HBM)
SMEM = pl.BlockSpec(memory_space=pltpu.SMEM)


def roomy(mebibytes):
    return pltpu.CompilerParams(vmem_limit_bytes=mebibytes * 1024 * 1024)


class Geometry:
    def __init__(self, size_ref, pair):
        parity = lax.broadcasted_iota(jnp.int32, (8, 128), 0) % 2
        high, broad, turned = (
            jnp.where(parity == 0, size_ref[pair * 6 + n], size_ref[pair * 6 + 3 + n])
            for n in range(3)
        )
        self.high = high
        self.count_two = (high * broad * C2).astype(f32)[:, :1]
        self.high3 = (high + 1) // 2
        broad3 = (broad + 1) // 2
        self.count_three = (self.high3 * broad3 * C3).astype(f32)[:, :1]
        place = lax.broadcasted_iota(jnp.int32, (LINE, 128), 0) // 2
        inside = lax.broadcasted_iota(jnp.int32, (LINE, 128), 0) < 2 * W3
        self.reach = []
        self.col_share = []
        for pc in range(2):
            column = 2 * place + pc
            self.reach.append(jnp.where(inside & (column < line(broad)), line(high), 0))
            edge = (column == 0) | (column == line(broad) - 1)
            self.col_share.append(jnp.where(edge, 0.5, 1.0 / 3.0))
        self.reach3 = jnp.where(inside & (place < line(broad3)), line(self.high3), 0)
        edge3 = (place == 0) | (place == line(broad3) - 1)
        self.col_share3 = jnp.where(edge3, 0.5, 1.0 / 3.0)
        self.flipped = jnp.concatenate([turned] * (STEP // 8), axis=0) > 0

    def share(self, plane, k):
        pr, pc = plane // 2, plane % 2
        return self.lines(4 * k + pr, 2, self.reach[pc], self.col_share[pc], self.high)

    def share3(self, k):
        return self.lines(2 * k, 1, self.reach3, self.col_share3, self.high3)

    def lines(self, row, stride, reach, col_share, height):
        parts = []
        for n in range(2):
            here = row + stride * n
            row_share = jnp.where((here == 0) | (here == height - 1), 0.5, 1.0 / 3.0)
            parts.append(jnp.where(here < reach, line(row_share) * col_share, 0.0))
        return jnp.concatenate(parts, axis=0)


def strip_place(pair, spot, strip_count):
    return lax.rem(pair * 8 + strip_count - 2 + spot, strip_count)


def each_image(size_ref, pair, visit):
    for image in range(2):
        way = size_ref[pair * 6 + 3 * image + 2]

        @pl.when(way == 0)
        def _():
            def one(r, carry):
                for plane in range(4):
                    row = 2 * r + plane // 2
                    strip = row // SR
                    there = pl.ds((row - strip * SR) * CW + plane % 2, W3, stride=2)
                    here = pl.ds(r * LINE + image, W3, stride=2)
                    visit(plane, here, image * STRIPS + strip, there)
                return carry

            lax.fori_loop(0, LINES, one, 0)

        @pl.when(way == 1)
        def _():
            def one(r, carry):
                for plane in range(4):
                    for strip in range(STRIPS):
                        first = (plane % 2 + strip * SR) % 2
                        count = (SR - first + 1) // 2
                        done = (strip * SR + first) // 2
                        column = 2 * r + plane // 2
                        there = pl.ds(first * CW + column, count, stride=2 * CW)
                        here = pl.ds(r * LINE + image + 2 * done, count, stride=2)
                        visit(plane, here, image * STRIPS + strip, there)
                return carry

            lax.fori_loop(0, LINES, one, 0)


def row_windows(col_ref, pc, k):
    both = col_ref[pc, step_rows(k, 1)] + col_ref[2 + pc, step_rows(k, 1)]
    return (both + col_ref[2 + pc, step_rows(k)], both + col_ref[pc, step_rows(k, 2)])


def put_col_windows(col_ref, pr, k, even, odd):
    both = even + odd
    col_ref[pr * 2, step_rows(k, 1)] = both + from_left(odd)
    col_ref[pr * 2 + 1, step_rows(k, 1)] = both + from_right(even)


def clear_edges(col_ref):
    zero_line = jnp.zeros((LINE, C2), f32)
    for plane in range(4):
        col_ref[plane, 0:LINE] = zero_line
        col_ref[plane, AREA + LINE : AREA + 2 * LINE] = zero_line


def entry_kernel(pairs, strip_count, piece_count, place_ref, size_ref, vec_two_ref, *refs):
    piece_refs, refs = refs[:piece_count], refs[piece_count:]
    x_out, inv_out, pool_out, mix_out, stat_out, image_ref, col_ref = refs
    pair = pl.program_id(0) if pairs > 1 else 0
    x_ref, inv_ref, pool_ref, mix_ref = (ref.at[0] for ref in (x_out, inv_out, pool_out, mix_out))
    shape = Geometry(size_ref, pair)
    gain1, bias1, scale1 = (vec_two_ref[n : n + 1] for n in range(3))
    clear_edges(col_ref)
    if piece_count > 1:
        half = piece_count // 2
        for n, ref in enumerate(piece_refs):
            source = place_ref[0] ^ (n // half + 2 * (n % half))
            spot = lax.rem(source + 2, 2 * STRIPS)
            first = 0 if n < half else ref.shape[0] - STRIP_ROWS
            image_ref[spot] = ref[first : first + STRIP_ROWS].astype(f32)
    else:
        for spot in range(2 * STRIPS):
            source = strip_place(pair, spot, strip_count)
            image_ref[spot] = piece_refs[0][source].astype(f32)

    def take_in(plane, here, spot, there):
        x_ref[plane, here] = image_ref[spot, there]

    each_image(size_ref, pair, take_in)

    def arrange(k, carry):
        total, square = carry
        rows = step_rows(k)
        for plane in range(4):
            share = shape.share(plane, k)
            inv_ref[plane, rows] = share
            values = jnp.where(share > 0.0, x_ref[plane, rows], 0.0)
            x_ref[plane, rows] = values
            total = total + fold(values)
            square = square + fold(values * values)
        return (total, square)

    nothing = jnp.zeros((8, C2), f32)
    total, square = sweep(arrange, (nothing, nothing))
    mean1, scaling1 = norm_terms(total, square, shape.count_two)
    factor1 = scaling1 * gain1
    shift1 = bias1 - mean1 * scaling1 * gain1

    def window_cols(k, carry):
        rows = step_rows(k)
        for pr in range(2):
            masked = []
            for pc in range(2):
                plane = pr * 2 + pc
                normal = rounded(affine(x_ref[plane, rows], factor1, shift1))
                masked.append(jnp.where(inv_ref[plane, rows] > 0.0, normal, 0.0))
            put_col_windows(col_ref, pr, k, *masked)
        return carry

    sweep(window_cols, 0)

    def mix(k, carry):
        total, square = carry
        rows = step_rows(k)
        for pc in range(2):
            windows = row_windows(col_ref, pc, k)
            for pr in range(2):
                plane = pr * 2 + pc
                values = x_ref[plane, rows]
                share = inv_ref[plane, rows]
                pooled = windows[pr] * share - rounded(affine(values, factor1, shift1))
                pooled = jnp.where(share > 0.0, pooled, 0.0)
                mixed = values + scale1 * pooled
                pool_ref[plane, rows] = pooled
                mix_ref[plane, rows] = mixed
                total = total + fold(mixed)
                square = square + fold(mixed * mixed)
        return (total, square)

    total, square = sweep(mix, (nothing, nothing))
    mean2, scaling2 = norm_terms(total, square, shape.count_two)
    for n, value in enumerate((mean1, scaling1, mean2, scaling2)):
        stat_out[0, n] = spread(value, 128)


def pair_specs(pairs, shapes, mode=None):
    if pairs == 1:
        return [VMEM_BLOCK] * len(shapes)
    return [
        pl.BlockSpec(
            (1,) + shape, lambda t, rank=len(shape): (t,) + (0,) * rank, pipeline_mode=mode
        )
        for shape in shapes
    ]


def whole_specs(pairs, shapes):
    if pairs == 1:
        return [VMEM_BLOCK] * len(shapes)
    return [
        pl.BlockSpec(
            shape,
            lambda t, rank=len(shape): (0,) * rank,
            pipeline_mode=pl.Buffered(1),
        )
        for shape in shapes
    ]


def pair_arrays(pairs, shapes, kinds):
    make = pltpu.VMEM if pairs == 1 else jax.ShapeDtypeStruct
    return [make((pairs,) + shape, kind) for shape, kind in zip(shapes, kinds)]


STATE = [(4, AREA, C2)] * 4 + [(4, 8, 128)]
BACK = [(4, AREA, C2)] * 2 + [(2, 8, 128)]


def run_entry(place, sizes, pieces, vec_two, strip_count):
    pairs = strip_count // 8
    if pairs == 1:
        pieces = held_in(pltpu.VMEM, *pieces)
    return pl.pallas_call(
        functools.partial(entry_kernel, pairs, strip_count, len(pieces)),
        grid=() if pairs == 1 else (pairs,),
        in_specs=[SMEM] * 2 + whole_specs(pairs, [array.shape for array in (vec_two, *pieces)]),
        out_specs=pair_specs(pairs, STATE),
        out_shape=pair_arrays(pairs, STATE, [f32] * 5),
        scratch_shapes=[
            pltpu.VMEM((2 * STRIPS, STRIP_ROWS, C2), f32),
            pltpu.VMEM((4, AREA + 2 * LINE, C2), f32),
        ],
        compiler_params=roomy(6 if pairs == 1 else 40),
        name="entry",
    )(place, sizes, vec_two, *pieces)


WEIGHTS = [(C2, HID2), (HID2, C2), (9 * C2, WIDE), (WIDE, HID3), (HID3, WIDE)]


def unpack_kernel(spans, slot_ref, *refs):
    piece_refs, refs = refs[: len(spans)], refs[len(spans) :]
    weights, gathered_ref = refs[:-1], refs[-1]
    done = 0
    for ref, (first, count) in zip(piece_refs, spans):
        blocks = ref[first : first + count * HALF].reshape(count, HALF, 128)
        gathered_ref[done : done + count] = blocks
        done += count
    left_half = lax.broadcasted_iota(jnp.int32, (HALF, 128), 1) < BS
    offset = 0
    for (rows, cols), ref in zip(SHAPES, weights):
        wide = cols // BS
        for rb in range(rows // BS):
            for cb in range(0, wide, 2):
                number = offset + rb * wide + cb
                first = gathered_ref[slot_ref[number]]
                turned = pltpu.roll(first, BS, 1)
                if cb + 1 < wide:
                    second = gathered_ref[slot_ref[number + 1]]
                    top = jnp.where(left_half, first, pltpu.roll(second, BS, 1))
                    low = jnp.where(left_half, turned, second)
                else:
                    top = jnp.where(left_half, first, 0.0)
                    low = jnp.where(left_half, turned, 0.0)
                place = slice(cb * BS, cb * BS + 128)
                ref[rb * BS : rb * BS + HALF, place] = top
                ref[rb * BS + HALF : rb * BS + BS, place] = low
        offset += rows // BS * wide
    weights[3][C3:, :] = jnp.zeros((WIDE - C3, HID3), bf16)


def run_unpack(slot_of, pieces, spans):
    slots = slot_of.shape[0]
    return pl.pallas_call(
        functools.partial(unpack_kernel, spans),
        in_specs=[SMEM] + [VMEM_BLOCK] * len(pieces),
        out_specs=[VMEM_BLOCK] * 5,
        out_shape=[pltpu.VMEM(shape, bf16) for shape in WEIGHTS],
        scratch_shapes=[pltpu.VMEM((slots, HALF, 128), bf16)],
        compiler_params=roomy(6),
        name="unpack",
    )(slot_of, *held_in(pltpu.VMEM, *pieces))


def main_kernel(
    pairs,
    strip_count,
    slots,
    near_place,
    far_place,
    size_ref,
    inv_in,
    mix_in,
    stat_in,
    goal_ref,
    vec_two_ref,
    vec_hid_two_ref,
    vec_three_ref,
    vec_hid_three_ref,
    w1_ref,
    w2_ref,
    we_ref,
    w3_ref,
    w4_ref,
    result_ref,
    zed_out,
    dx_out,
    mean_out,
    near_ref,
    far_ref,
    flat_ref,
    zed_ref,
    hid_ref,
    u_ref,
    g_ref,
    h_ref,
    dy_ref,
    patch_ref,
    dpatch_ref,
    inv3_ref,
    e_ref,
    col3_ref,
    pool3_ref,
    mix3_ref,
    dx3_ref,
    hid3_ref,
    dhid3_ref,
    u3_ref,
    g3_ref,
    h3_ref,
    dy3_ref,
    dpre_ref,
    gw1_ref,
    gw2_ref,
    gwe_ref,
    gw3_ref,
    gw4_ref,
    acc_two,
    acc_hid_two,
    acc_three,
    acc_hid_three,
):
    pair = pl.program_id(0) if pairs > 1 else 0
    grads = [gw1_ref, gw2_ref, gwe_ref, gw3_ref, gw4_ref]
    inv_ref, mix_ref, stat_ref = (ref.at[0] for ref in (inv_in, mix_in, stat_in))
    back_ref, dx_ref = zed_out.at[0], dx_out.at[0]
    left_half = lax.broadcasted_iota(jnp.int32, (HALF, 128), 1) < BS

    def at_pair(number, act):
        if pairs == 1:
            act()
        else:
            pl.when(pair == number)(act)

    def begin():
        acc_two[...] = jnp.zeros(acc_two.shape, f32)
        acc_hid_two[...] = jnp.zeros(acc_hid_two.shape, f32)
        acc_three[...] = jnp.zeros(acc_three.shape, f32)
        acc_hid_three[...] = jnp.zeros(acc_hid_three.shape, f32)

    at_pair(0, begin)
    shape = Geometry(size_ref, pair)
    count_two, count_three, flipped = shape.count_two, shape.count_three, shape.flipped
    nothing = jnp.zeros((8, C2), f32)
    nothing3 = jnp.zeros((8, WIDE), f32)
    gain2, bias2, scale2, out_bias = (vec_two_ref[n : n + 1] for n in range(3, 7))
    embed_bias, gain3, bias3, scale3 = (vec_three_ref[n : n + 1] for n in range(4))
    gain4, bias4, scale4, out_bias3 = (vec_three_ref[n : n + 1] for n in range(4, 8))
    mean2, scaling2 = stat_ref[2], stat_ref[3]
    factor2 = scaling2 * gain2
    shift2 = bias2 - mean2 * scaling2 * gain2
    for plane in range(4):
        zed_ref[plane, 0:LINE] = jnp.zeros((LINE, C2), f32)
    col3_ref[0:LINE] = jnp.zeros((LINE, WIDE), f32)
    col3_ref[AREA + LINE : AREA + 2 * LINE] = jnp.zeros((LINE, WIDE), f32)

    def put_block(number, block):
        near_ref[near_place[number]] = block
        far_ref[far_place[number]] = block

    def pack_blocks(matrices):
        offsets = [0]
        for rows, cols in SHAPES:
            offsets.append(offsets[-1] + rows // BS * (cols // BS))
        for which in matrices:
            (rows, cols), ref = SHAPES[which], grads[which]
            wide = cols // BS
            for rb in range(rows // BS):
                for cb in range(0, wide, 2):
                    number = offsets[which] + rb * wide + cb
                    at = slice(cb * BS, cb * BS + 128)
                    top = ref[rb * BS : rb * BS + HALF, at].astype(bf16)
                    low = ref[rb * BS + HALF : rb * BS + BS, at].astype(bf16)
                    put_block(number, jnp.where(left_half, top, pltpu.roll(low, BS, 1)))
                    if cb + 1 < wide:
                        put_block(number + 1, jnp.where(left_half, pltpu.roll(top, BS, 1), low))

    def plane_rows(plane):
        return slice(plane * AREA, plane * AREA + AREA)

    def begin_plane(plane):
        low = affine(mix_ref[plane], factor2, shift2).astype(bf16)
        h_ref[plane_rows(plane)] = low
        hid_ref[plane % 2] = product(low, w1_ref[...])

    begin_plane(0)
    for plane in range(4):
        if plane < 3:
            begin_plane(plane + 1)
        for k in range(STEPS):
            rows = step_rows(k)
            flat = slice(plane * AREA + k * STEP, plane * AREA + k * STEP + STEP)
            for at in range(0, HID2, 128):
                lanes = slice(at, at + 128)
                active, slope = gelu_pair(hid_ref[plane % 2, rows, lanes] + vec_hid_two_ref[:, lanes])
                u_ref[flat, lanes] = active.astype(bf16)
                g_ref[flat, lanes] = slope.astype(bf16)
        out = product(u_ref[plane_rows(plane)], w2_ref[...]) + out_bias
        zed = jnp.where(inv_ref[plane] > 0.0, mix_ref[plane] + scale2 * out, 0.0)
        zed_ref[plane, LINE : LINE + AREA] = rounded(zed)

    def patches(k, carry):
        rows = step_rows(k)
        taps = []
        for ky in range(3):
            pr = (0 if ky == 1 else 1) * 2
            source = step_rows(k, 0 if ky == 0 else 1)
            even = zed_ref[pr, source]
            odd = zed_ref[pr + 1, source]
            taps.append((from_left(odd), even, odd))
        for ky in range(3):
            for kx in range(3):
                at = (3 * ky + kx) * C2
                tap = taps[ky][kx]
                if ky != kx:
                    tap = jnp.where(flipped, taps[kx][ky], tap)
                patch_ref[rows, at : at + C2] = tap.astype(bf16)
        return carry

    sweep(patches, 0)
    e_ref[...] = product(patch_ref[...], we_ref[...])

    def embed(k, carry):
        total, square = carry
        rows = step_rows(k)
        share = shape.share3(k)
        inv3_ref[rows] = share
        out = jnp.where(widen(share) > 0.0, e_ref[rows] + embed_bias, 0.0)
        e_ref[rows] = out
        return (total + fold(out), square + fold(out * out))

    total, square = sweep(embed, (nothing3, nothing3))
    mean3, scaling3 = norm_terms(total, square, count_three)
    factor3 = scaling3 * gain3
    shift3 = bias3 - mean3 * scaling3 * gain3

    def window_cols3(k, carry):
        rows = step_rows(k)
        normal = rounded(affine(e_ref[rows], factor3, shift3))
        masked = jnp.where(widen(inv3_ref[rows]) > 0.0, normal, 0.0)
        col3_ref[step_rows(k, 1)] = masked + from_left(masked) + from_right(masked)
        return carry

    sweep(window_cols3, 0)

    def row_windows3(k):
        return col3_ref[step_rows(k)] + col3_ref[step_rows(k, 1)] + col3_ref[step_rows(k, 2)]

    def mix3(k, carry):
        total, square = carry
        rows = step_rows(k)
        values = e_ref[rows]
        share = widen(inv3_ref[rows])
        pooled = row_windows3(k) * share - rounded(affine(values, factor3, shift3))
        pooled = jnp.where(share > 0.0, pooled, 0.0)
        mixed = values + scale3 * pooled
        pool3_ref[rows] = pooled
        mix3_ref[rows] = mixed
        return (total + fold(mixed), square + fold(mixed * mixed))

    total, square = sweep(mix3, (nothing3, nothing3))
    mean4, scaling4 = norm_terms(total, square, count_three)
    factor4 = scaling4 * gain4
    shift4 = bias4 - mean4 * scaling4 * gain4
    normal4 = (spread(scaling4, WIDE), spread(-mean4 * scaling4, WIDE))

    def prepare3(k, d_bias):
        rows = step_rows(k)
        h3_ref[rows] = affine(mix3_ref[rows], factor4, shift4).astype(bf16)
        goal = goal_ref[0, rows].astype(f32)
        goal = jnp.where(widen(inv3_ref[rows]) > 0.0, goal, 0.0)
        low_goal = (scale4 * goal).astype(bf16)
        dy3_ref[rows] = low_goal
        return d_bias + fold(low_goal.astype(f32))

    acc_three[7] += sweep(prepare3, nothing3)

    def keep(ref, value, place=slice(None)):
        if pairs == 1:
            ref[place] = value.astype(ref.dtype)
        else:

            @pl.when(pair == 0)
            def _():
                ref[place] = value

            @pl.when(pair > 0)
            def _():
                ref[place] += value

    def begin_chunk(at):
        lanes = slice(at, at + 256)
        hid3_ref[:, lanes] = product(h3_ref[...], w3_ref[:, lanes])
        dhid3_ref[:, lanes] = product_nt(dy3_ref[...], w4_ref[lanes])

    begin_chunk(0)
    for at in range(0, HID3, 256):
        if at + 256 < HID3:
            begin_chunk(at + 256)
        for lane in (at, at + 128):
            lanes = slice(lane, lane + 128)
            total = nothing
            for k in range(STEPS):
                rows = step_rows(k)
                active, slope = gelu_pair(hid3_ref[rows, lanes] + vec_hid_three_ref[:, lanes])
                u3_ref[rows, lanes] = active.astype(bf16)
                low = (slope * dhid3_ref[rows, lanes]).astype(bf16)
                g3_ref[rows, lanes] = low
                total = total + fold(low.astype(f32))
            acc_hid_three[:, lanes] += total
        lanes = slice(at, at + 256)
        out = product(u3_ref[:, lanes], w4_ref[lanes])
        d_low = product_nt(g3_ref[:, lanes], w3_ref[:, lanes])
        result_ref[0] = out if at == 0 else result_ref[0] + out
        dx3_ref[...] = d_low if at == 0 else dx3_ref[...] + d_low
        keep(gw3_ref, product_tn(h3_ref[...], g3_ref[:, lanes]), (slice(None), lanes))
        keep(gw4_ref, product_tn(u3_ref[:, lanes], dy3_ref[...]), lanes)

    def finish3(k, carry):
        d_scale, d_shift, d_gain = carry
        rows = step_rows(k)
        valid = widen(inv3_ref[rows]) > 0.0
        mixed = mix3_ref[rows]
        out = jnp.where(valid, result_ref[0, rows] + out_bias3, 0.0)
        result_ref[0, rows] = mixed + scale4 * out
        d_scale = d_scale + fold(out * goal_ref[0, rows].astype(f32))
        d_low = dx3_ref[rows]
        normal = affine(mixed, *normal4)
        return (d_scale, d_shift + fold(d_low), d_gain + fold(d_low * normal))

    d_scale, d_shift, d_gain = sweep(finish3, (nothing3, nothing3, nothing3))
    acc_three[6] += d_scale
    acc_three[5] += d_shift
    acc_three[4] += d_gain
    mean_shift = by_image(d_shift * gain4) / count_three
    mean_gain = by_image(d_gain * gain4) / count_three
    back_gain4 = scaling4 * gain4
    back_mean4 = spread(-scaling4 * mean_shift, WIDE)
    back_normal4 = spread(scaling4 * mean_gain, WIDE)

    def unmix3(k, d_scale):
        rows = step_rows(k)
        share = widen(inv3_ref[rows])
        valid = share > 0.0
        normal = affine(mix3_ref[rows], *normal4)
        back = affine(dx3_ref[rows], back_gain4, back_mean4) - scaled(normal, back_normal4)
        d_mixed = jnp.where(valid, back + goal_ref[0, rows].astype(f32), 0.0)
        dx3_ref[rows] = d_mixed
        d_scale = d_scale + fold(pool3_ref[rows] * d_mixed)
        weighted = scale3 * d_mixed * share
        col3_ref[step_rows(k, 1)] = weighted + from_left(weighted) + from_right(weighted)
        return d_scale

    acc_three[3] += sweep(unmix3, nothing3)
    normal3 = (spread(scaling3, WIDE), spread(-mean3 * scaling3, WIDE))

    def unpool3(k, carry):
        d_shift, d_gain = carry
        rows = step_rows(k)
        valid = widen(inv3_ref[rows]) > 0.0
        d_normal = jnp.where(valid, row_windows3(k) - scale3 * dx3_ref[rows], 0.0)
        pool3_ref[rows] = d_normal
        normal = affine(e_ref[rows], *normal3)
        return (d_shift + fold(d_normal), d_gain + fold(d_normal * normal))

    d_shift, d_gain = sweep(unpool3, (nothing3, nothing3))
    acc_three[2] += d_shift
    acc_three[1] += d_gain
    mean_shift = by_image(d_shift * gain3) / count_three
    mean_gain = by_image(d_gain * gain3) / count_three
    back_gain3 = scaling3 * gain3
    back_mean3 = spread(-scaling3 * mean_shift, WIDE)
    back_normal3 = spread(scaling3 * mean_gain, WIDE)

    def unnorm3(k, d_bias):
        rows = step_rows(k)
        valid = widen(inv3_ref[rows]) > 0.0
        normal = affine(e_ref[rows], *normal3)
        back = affine(pool3_ref[rows], back_gain3, back_mean3) - scaled(normal, back_normal3)
        low = jnp.where(valid, dx3_ref[rows] + back, 0.0).astype(bf16)
        dpre_ref[rows] = low
        return d_bias + fold(low.astype(f32))

    acc_three[0] += sweep(unnorm3, nothing3)
    keep(gwe_ref, product_tn(patch_ref[...], dpre_ref[...]))
    dpatch_ref[0:AREA] = product_nt(dpre_ref[...], we_ref[...])
    dpatch_ref[AREA : AREA + LINE] = jnp.zeros((LINE, 9 * C2), f32)

    def gather_back(k, carry):
        rows = step_rows(k)

        def tap(ky, kx, source):
            at = (3 * ky + kx) * C2
            value = dpatch_ref[source, at : at + C2]
            if ky != kx:
                at = (3 * kx + ky) * C2
                value = jnp.where(flipped, dpatch_ref[source, at : at + C2], value)
            return value

        sources = []
        for ky in range(3):
            source = step_rows(k, 1 if ky == 0 else 0)
            sources.append(
                (tap(ky, 1, source), tap(ky, 2, source) + from_right(tap(ky, 0, source)))
            )
        for pc in range(2):
            for pr, value in ((0, sources[1][pc]), (1, sources[2][pc] + sources[0][pc])):
                plane = pr * 2 + pc
                valid = inv_ref[plane, rows] > 0.0
                back_ref[plane, rows] = jnp.where(valid, rounded(value), 0.0)
        return carry

    sweep(gather_back, 0)

    if pairs == 1:
        pack_blocks(range(2, 5))

    normal2 = (spread(scaling2, C2), spread(-mean2 * scaling2, C2))

    def begin_back(plane):
        low_goal = (scale2 * back_ref[plane]).astype(bf16)
        dy_ref[plane_rows(plane)] = low_goal
        hid_ref[plane % 2] = product_nt(low_goal, w2_ref[...])
        return fold(low_goal.astype(f32))

    d_out_bias = begin_back(0)
    d_shift, d_gain = nothing, nothing
    sums = [nothing] * (HID2 // 128)
    new_gw1, new_gw2 = None, None
    for plane in range(4):
        if plane < 3:
            d_out_bias = d_out_bias + begin_back(plane + 1)
        for k in range(STEPS):
            rows = step_rows(k)
            part = slice(plane * AREA + k * STEP, plane * AREA + k * STEP + STEP)
            for n, at in enumerate(range(0, HID2, 128)):
                lanes = slice(at, at + 128)
                low = g_ref[part, lanes].astype(f32) * hid_ref[plane % 2, rows, lanes]
                low = low.astype(bf16)
                g_ref[part, lanes] = low
                sums[n] = sums[n] + fold(low.astype(f32))
        flat = plane_rows(plane)
        d_low = product_nt(g_ref[flat], w1_ref[...])
        dx_ref[plane] = d_low
        d_shift = d_shift + fold(d_low)
        d_gain = d_gain + fold(d_low * affine(mix_ref[plane], *normal2))
        part_gw1 = product_tn(h_ref[flat], g_ref[flat])
        part_gw2 = product_tn(dy_ref[flat], u_ref[flat])
        new_gw1 = part_gw1 if plane == 0 else new_gw1 + part_gw1
        new_gw2 = part_gw2 if plane == 0 else new_gw2 + part_gw2
    new_gw2 = new_gw2.T
    for n, value in enumerate(sums):
        acc_hid_two[:, n * 128 : n * 128 + 128] += value
    acc_two[6] += d_out_bias
    acc_two[4] += d_shift
    acc_two[3] += d_gain
    mean_out[0, 0] = spread(by_image(d_shift * gain2) / count_two, 128)
    mean_out[0, 1] = spread(by_image(d_gain * gain2) / count_two, 128)
    keep(gw1_ref, new_gw1)
    keep(gw2_ref, new_gw2)
    d_scale = fold(w2_ref[...].astype(f32) * new_gw2) + out_bias * d_out_bias
    acc_two[5] += d_scale / scale2

    def finish():
        if pairs > 1:
            pack_blocks(range(5))
        else:
            pack_blocks(range(2))

        def filler(number, carry):
            put_block(number, jnp.zeros((HALF, 128), bf16))
            return carry

        lax.fori_loop(USED, slots, filler, 0)

        flat_ref[...] = jnp.zeros(flat_ref.shape, f32)

        def put(at, total, length):
            if at % 128:
                room = jnp.zeros((8, 128), f32)
                if total.shape[1] < length + BS:
                    total = jnp.concatenate([total, room], axis=1)
                total = pltpu.roll(total, BS, 1)
            whole = jnp.sum(total, axis=0, keepdims=True)
            done = -(at % 128)
            row = at // 128
            lane = 0
            while done < length:
                first = max(0, -done)
                last = min(128, length - done)
                flat_ref[row : row + 1, first:last] = whole[:, lane + first : lane + last]
                done += 128
                lane += 128
                row += 1

        at = 3 * C2
        for n in range(3, 6):
            put(at, acc_two[n], C2)
            at += C2
        put(at, acc_hid_two[...], HID2)
        at += HID2
        put(at, acc_two[6], C2)
        at += C2
        for n in range(7):
            put(at, acc_three[n], C3)
            at += C3
        put(at, acc_hid_three[...], HID3)
        at += HID3
        put(at, acc_three[7], C3)

    at_pair(pairs - 1, finish)


def run_main(places, sizes, state, goal, vectors, weights, strip_count):
    pairs = goal.shape[0]
    slots = places[0].shape[0]
    half = slots // 2 + 1
    if pairs == 1:
        state = held_in(pltpu.VMEM, *state)
    weights = held_in(pltpu.VMEM, *weights)
    _, inv, _, mix, stat = state
    state_shapes = [STATE[1], STATE[3], STATE[4]]
    grad_kind = bf16 if pairs == 1 else f32
    wide_f32 = pltpu.VMEM((AREA, WIDE), f32)
    wide_bf16 = pltpu.VMEM((AREA, WIDE), bf16)
    scratch = [
        pltpu.VMEM((4, AREA + LINE, C2), f32),
        pltpu.VMEM((2, AREA, HID2), f32),
        pltpu.VMEM((4 * AREA, HID2), bf16),
        pltpu.VMEM((4 * AREA, HID2), bf16),
        pltpu.VMEM((4 * AREA, C2), bf16),
        pltpu.VMEM((4 * AREA, C2), bf16),
        pltpu.VMEM((AREA, 9 * C2), bf16),
        pltpu.VMEM((AREA + LINE, 9 * C2), f32),
        pltpu.VMEM((AREA, 128), f32),
        wide_f32,
        pltpu.VMEM((AREA + 2 * LINE, WIDE), f32),
        wide_f32,
        wide_f32,
        wide_f32,
        pltpu.VMEM((AREA, HID3), f32),
        pltpu.VMEM((AREA, HID3), f32),
        pltpu.VMEM((AREA, HID3), bf16),
        pltpu.VMEM((AREA, HID3), bf16),
        wide_bf16,
        wide_bf16,
        wide_bf16,
        pltpu.VMEM((C2, HID2), grad_kind),
        pltpu.VMEM((HID2, C2), grad_kind),
        pltpu.VMEM((9 * C2, WIDE), grad_kind),
        pltpu.VMEM((WIDE, HID3), grad_kind),
        pltpu.VMEM((HID3, WIDE), grad_kind),
        pltpu.VMEM((7, 8, C2), f32),
        pltpu.VMEM((8, HID2), f32),
        pltpu.VMEM((8, 8, WIDE), f32),
        pltpu.VMEM((8, HID3), f32),
    ]
    out_shapes = [(half, HALF, 128), (half, HALF, 128), (VEC_BLOCKS * HALF, 128)]
    make = pltpu.VMEM if pairs == 1 else jax.ShapeDtypeStruct
    return pl.pallas_call(
        functools.partial(main_kernel, pairs, strip_count, slots),
        grid=() if pairs == 1 else (pairs,),
        in_specs=[SMEM] * 3
        + pair_specs(pairs, state_shapes + [goal.shape[1:]], pl.Buffered(1))
        + whole_specs(pairs, [vector.shape for vector in vectors])
        + [VMEM_BLOCK] * 5,
        out_specs=pair_specs(pairs, [(AREA, WIDE)] + BACK) + whole_specs(pairs, out_shapes),
        out_shape=pair_arrays(pairs, [(AREA, WIDE)] + BACK, [f32] * 4)
        + [make(shape, kind) for shape, kind in zip(out_shapes, (bf16, bf16, f32))],
        scratch_shapes=scratch,
        compiler_params=pltpu.CompilerParams(
            vmem_limit_bytes=(40 if pairs == 1 else 56) * 1024 * 1024,
            fuse_transposed_lhs_in_matmul=True,
        ),
        name="blocks",
    )(*places, sizes, inv, mix, stat, goal, *vectors, *weights)


def exit_kernel(
    pairs,
    strip_count,
    size_ref,
    x_in,
    inv_in,
    pool_in,
    mix_in,
    stat_in,
    zed_in,
    dx_in,
    mean_in,
    flat_ref,
    vec_two_ref,
    payload_hbm,
    vector_ref,
    payload_ref,
    image_ref,
    col_ref,
    dx_ref,
    back_ref,
    acc_ref,
    sem,
):
    pair = pl.program_id(0) if pairs > 1 else 0
    x_ref, inv_ref, pool_ref, mix_ref, stat_ref, zed_ref, low_ref, mean_ref = (
        ref.at[0] for ref in (x_in, inv_in, pool_in, mix_in, stat_in, zed_in, dx_in, mean_in)
    )
    shape = Geometry(size_ref, pair)
    count_two = shape.count_two
    gain1, bias1, scale1, gain2 = (vec_two_ref[n : n + 1] for n in range(4))
    mean1, scaling1, mean2, scaling2 = (stat_ref[n] for n in range(4))
    normal2 = (scaling2, -mean2 * scaling2)
    clear_edges(col_ref)
    nothing = jnp.zeros((8, C2), f32)
    back_gain2 = scaling2 * gain2
    back_mean2 = -scaling2 * mean_ref[0]
    back_normal2 = scaling2 * mean_ref[1]

    if pairs > 1:

        @pl.when(pair == 0)
        def _():
            acc_ref[...] = jnp.zeros(acc_ref.shape, f32)

    def add_up(n, total):
        acc_ref[n] = total if pairs == 1 else acc_ref[n] + total

    def unmix(k, d_scale):
        rows = step_rows(k)
        for pr in range(2):
            weighted = []
            for pc in range(2):
                plane = pr * 2 + pc
                share = inv_ref[plane, rows]
                normal = affine(mix_ref[plane, rows], *normal2)
                back = affine(low_ref[plane, rows], back_gain2, back_mean2)
                back = back - scaled(normal, back_normal2)
                d_mixed = jnp.where(share > 0.0, zed_ref[plane, rows] + back, 0.0)
                dx_ref[plane, rows] = d_mixed
                d_scale = d_scale + fold(pool_ref[plane, rows] * d_mixed)
                weighted.append(scale1 * d_mixed * share)
            put_col_windows(col_ref, pr, k, *weighted)
        return d_scale

    add_up(2, sweep(unmix, nothing))
    normal1 = (spread(scaling1, C2), spread(-mean1 * scaling1, C2))

    def unpool(k, carry):
        d_shift, d_gain = carry
        rows = step_rows(k)
        for pc in range(2):
            windows = row_windows(col_ref, pc, k)
            for pr in range(2):
                plane = pr * 2 + pc
                valid = inv_ref[plane, rows] > 0.0
                d_normal = windows[pr] - scale1 * dx_ref[plane, rows]
                d_normal = jnp.where(valid, d_normal, 0.0)
                back_ref[plane, rows] = d_normal
                normal = affine(x_ref[plane, rows], *normal1)
                d_shift = d_shift + fold(d_normal)
                d_gain = d_gain + fold(d_normal * normal)
        return (d_shift, d_gain)

    d_shift, d_gain = sweep(unpool, (nothing, nothing))
    add_up(1, d_shift)
    add_up(0, d_gain)
    mean_shift = by_image(d_shift * gain1) / count_two
    mean_gain = by_image(d_gain * gain1) / count_two
    back_gain1 = scaling1 * gain1
    back_mean1 = spread(-scaling1 * mean_shift, C2)
    back_normal1 = spread(scaling1 * mean_gain, C2)

    def unnorm(k, carry):
        rows = step_rows(k)
        for plane in range(4):
            normal = affine(x_ref[plane, rows], *normal1)
            back = affine(back_ref[plane, rows], back_gain1, back_mean1)
            back = back - scaled(normal, back_normal1)
            valid = inv_ref[plane, rows] > 0.0
            dx_ref[plane, rows] = jnp.where(valid, dx_ref[plane, rows] + back, 0.0)
        return carry

    sweep(unnorm, 0)

    def give_back(plane, here, spot, there):
        image_ref[spot, there] = dx_ref[plane, here]

    image_ref[...] = jnp.zeros(image_ref.shape, f32)
    each_image(size_ref, pair, give_back)

    for spot in range(2 * STRIPS):
        target = strip_place(pair, spot, strip_count)
        for within in range(SR):
            rows = slice(within * CW, within * CW + CW)
            payload_ref[target, within] = image_ref[spot, rows].astype(bf16)

    def finish():
        copy = pltpu.make_async_copy(payload_ref, payload_hbm, sem)
        copy.start()
        vector_ref[...] = flat_ref[...]
        for n in range(3):
            vector_ref[n : n + 1] = jnp.sum(acc_ref[n], axis=0, keepdims=True)
        copy.wait()

    if pairs == 1:
        finish()
    else:
        pl.when(pair == pairs - 1)(finish)


def run_exit(sizes, state, back, flat, vec_two, strip_count):
    pairs = strip_count // 8
    payload = (strip_count, SR, CW, C2)
    make = pltpu.VMEM if pairs == 1 else jax.ShapeDtypeStruct
    plane_f32 = pltpu.VMEM((4, AREA, C2), f32)
    arrays = [*state, *back]
    if pairs == 1:
        arrays = held_in(pltpu.VMEM, *arrays)
    return pl.pallas_call(
        functools.partial(exit_kernel, pairs, strip_count),
        grid=() if pairs == 1 else (pairs,),
        in_specs=[SMEM]
        + pair_specs(pairs, STATE + BACK, pl.Buffered(1))
        + whole_specs(pairs, [flat.shape, vec_two.shape]),
        out_specs=[HBM] + whole_specs(pairs, [flat.shape]),
        out_shape=[pltpu.HBM(payload, bf16), make(flat.shape, f32)],
        scratch_shapes=[
            pltpu.VMEM(payload, bf16),
            pltpu.VMEM((2 * STRIPS, STRIP_ROWS, C2), f32),
            pltpu.VMEM((4, AREA + 2 * LINE, C2), f32),
            plane_f32,
            plane_f32,
            pltpu.VMEM((3, 8, C2), f32),
            pltpu.SemaphoreType.DMA,
        ],
        compiler_params=roomy(8 if pairs == 1 else 40),
        name="exit",
    )(sizes, *arrays, flat, vec_two)


def dense_blocks(values):
    return jnp.concatenate([values[:, :HALF], values[:, HALF:]], axis=2).astype(bf16)


def pack_kernel(master_ref, dense_ref):
    dense_ref[...] = dense_blocks(master_ref[...])


def pack(master):
    owned = master.shape[0]
    return pl.pallas_call(
        pack_kernel,
        out_shape=jax.ShapeDtypeStruct((owned, HALF, 2 * BS), bf16),
        name="pack",
    )(master)


def pack_pieces_kernel(place_ref, master_hbm, pixel_hbm, *refs):
    out_refs, (wide_ref, master_ref, pixel_ref, sem) = refs[:-4], refs[-4:]
    owned = master_ref.shape[0]
    slots = pixel_ref.shape[2]
    copies = [pltpu.make_async_copy(pixel_hbm, pixel_ref, sem.at[0])]
    parts = [(0, owned // 2), (owned // 2, owned - owned // 2)]
    for n, part in enumerate(parts):
        copies.append(
            pltpu.make_async_copy(
                master_hbm.at[pl.ds(*part)], master_ref.at[pl.ds(*part)], sem.at[1 + n]
            )
        )
    for copy in copies:
        copy.start()
    copies[0].wait()

    def widen_row(row, carry):
        start = pl.multiple_of(row * CW * slots, 8)
        values = pixel_ref[row].astype(f32).reshape(CW * slots, C2)
        wide_ref[pl.ds(start, CW * slots)] = values
        return carry

    lax.fori_loop(0, SR, widen_row, 0)
    for k, ref in enumerate(out_refs):
        for other in range(2):
            slot = place_ref[0] ^ (2 * k + other)
            first = other * (ref.shape[0] - STRIP_ROWS)
            strip = wide_ref[pl.ds(slot, STRIP_ROWS, stride=slots)]
            ref[first : first + STRIP_ROWS] = strip.astype(bf16)
    for (first, count), copy in zip(parts, copies[1:]):
        copy.wait()
        dense = dense_blocks(master_ref[first : first + count]).reshape(count * HALF, 2 * BS)
        start = STRIP_ROWS + first * HALF
        for ref in out_refs[:3]:
            ref[start : start + count * HALF] = dense


def pack_pieces(place, master, pixels):
    slots = pixels.shape[2]
    rows = master.shape[0] * HALF
    shapes = [(rows + 2 * STRIP_ROWS, 2 * BS)] * 3 + [(2 * STRIP_ROWS, 2 * BS)]
    return pl.pallas_call(
        pack_pieces_kernel,
        in_specs=[SMEM] + [HBM] * 2,
        out_specs=[VMEM_BLOCK] * 4,
        out_shape=[pltpu.VMEM(shape, bf16) for shape in shapes],
        scratch_shapes=[
            pltpu.VMEM((STRIP_ROWS * slots, C2), f32),
            pltpu.VMEM(master.shape, f32),
            pltpu.VMEM(pixels.shape, bf16),
            pltpu.SemaphoreType.DMA((3,)),
        ],
        compiler_params=roomy(12),
        name="pack",
    )(place, *held_in(pltpu.HBM, master, pixels))


def fold_pair_kernel(near_ref, got_ref, own_ref, *part_refs):
    share = own_ref.shape[0]

    def one(n, carry):
        for k in range(len(part_refs) + 1):
            total = near_ref[k * share + n].astype(f32) + got_ref[k * share + n].astype(f32)
            if k == 0:
                own_ref[n] = total
            else:
                part_refs[k - 1][n] = total.astype(bf16)
        return carry

    lax.fori_loop(0, share, one, 0, unroll=4)


def fold_pair(near, got, groups):
    shape = ((near.shape[0] - 1) // groups,) + near.shape[1:]
    return pl.pallas_call(
        fold_pair_kernel,
        in_specs=[VMEM_BLOCK] * 2,
        out_specs=[VMEM_BLOCK] * groups,
        out_shape=[pltpu.VMEM(shape, f32)] + [pltpu.VMEM(shape, bf16)] * (groups - 1),
        compiler_params=roomy(4),
        name="fold_pair",
    )(*held_in(pltpu.VMEM, near, got))


def fold_tile_kernel(pieces, spot_ref, *refs):
    piece_refs, refs = refs[:pieces], refs[pieces:]
    vector_refs, refs = refs[:pieces], refs[pieces:]
    out_refs, sum_ref = refs[:-1], refs[-1]
    groups = len(out_refs)
    share = out_refs[0].shape[0]
    owned = piece_refs[0].shape[0]
    total = vector_refs[0][...]
    for ref in vector_refs[1:]:
        total = total + ref[...]
    for n in range(sum_ref.shape[0]):
        sum_ref[n] = jnp.zeros((HALF, 128), f32)
    for n in range(VEC_BLOCKS):
        sum_ref[n] = total[n * HALF : (n + 1) * HALF]

    def one(n, carry):
        for k, out_ref in enumerate(out_refs):
            number = lax.rem(spot_ref[0] + k, groups) * share + n
            block = jnp.minimum(number, owned - 1)
            total = piece_refs[0][block].astype(f32)
            for ref in piece_refs[1:]:
                total = total + ref[block].astype(f32)
            rest = sum_ref[jnp.maximum(number - owned, 0)]
            out_ref[n] = jnp.where(number < owned, total, rest).astype(out_ref.dtype)
        return carry

    lax.fori_loop(0, share, one, 0, unroll=share <= 16)


def fold_tile(spot, pieces, vectors, extra, groups):
    shape = ((pieces[0].shape[0] + extra) // groups,) + pieces[0].shape[1:]
    return pl.pallas_call(
        functools.partial(fold_tile_kernel, len(pieces)),
        in_specs=[SMEM] + [VMEM_BLOCK] * (len(pieces) + len(vectors)),
        out_specs=[VMEM_BLOCK] * groups,
        out_shape=[pltpu.VMEM(shape, f32)] + [pltpu.VMEM(shape, bf16)] * (groups - 1),
        scratch_shapes=[pltpu.VMEM((extra, HALF, 128), f32)],
        compiler_params=roomy(8),
        name="fold_tile",
    )(spot, *held_in(pltpu.VMEM, *pieces, *vectors))


def fold_batch_kernel(owned, vector_weight, spot_ref, *refs):
    part_refs, (total_ref, norm_ref) = refs[:-2], refs[-2:]
    share = total_ref.shape[0]
    square = jnp.zeros((8, 128), f32)
    for n in range(share):
        total = part_refs[0][n].astype(f32)
        for ref in part_refs[1:]:
            total = total + ref[n].astype(f32)
        total_ref[n] = total.astype(bf16)
        weight = jnp.where(spot_ref[0] * share + n < owned, 1.0, vector_weight)
        square = square + weight * fold(total * total)
    square = jnp.sum(jnp.sum(square, axis=1, keepdims=True), axis=0, keepdims=True)
    norm_ref[...] = jnp.broadcast_to(square[None], norm_ref.shape)


def fold_batch(spot, parts, owned, tile_count):
    count = tile_count * len(parts)
    return pl.pallas_call(
        functools.partial(fold_batch_kernel, owned, 1.0 / tile_count),
        in_specs=[SMEM] + [VMEM_BLOCK] * len(parts),
        out_specs=[VMEM_BLOCK] * 2,
        out_shape=[pltpu.VMEM(parts[0].shape, bf16), pltpu.VMEM((count, 1, 128), f32)],
        name="fold_batch",
    )(spot, *held_in(pltpu.VMEM, *parts))


def update_kernel(owned, groups, spot_ref, norm_ref, *refs):
    quarters, refs = refs[:groups], refs[groups:]
    stat_hbm, out_hbm, (vector_ref, clip_ref), refs = refs[:5], refs[5:10], refs[10:12], refs[12:]
    stat_refs, out_refs, (in_sem, out_sem) = refs[:5], refs[5:10], refs[10:]
    master_ref, left_stat_ref, right_stat_ref, left_root_ref, right_root_ref = stat_refs
    grad_ref, left_ref, right_ref, new_ref, copy_ref = out_refs
    share = quarters[0].shape[0]
    spans = spans_of(owned)

    def copies_of(sources, targets, sems):
        return [
            [
                pltpu.make_async_copy(
                    source.at[pl.ds(*span)], target.at[pl.ds(*span)], sems.at[5 * n + k]
                )
                for k, (source, target) in enumerate(zip(sources, targets))
            ]
            for n, span in enumerate(spans)
        ]

    copies_in = copies_of(stat_hbm, stat_refs, in_sem)
    copies_out = copies_of(out_refs, out_hbm, out_sem)
    for copies in copies_in:
        for copy in copies:
            copy.start()
    norm = jnp.sqrt(jnp.sum(norm_ref[...], axis=0))
    factor = jnp.minimum(1.0, clip_limit / norm)
    left_half = lax.broadcasted_iota(jnp.int32, (HALF, 128), 1) < BS

    def summed(number):
        source = number // share
        local = number - source * share
        turn = lax.rem(spot_ref[0] - source + groups, groups)
        value = quarters[0][local].astype(f32)
        for k in range(1, groups):
            value = jnp.where(turn == k, quarters[k][local].astype(f32), value)
        return value * factor

    def side_by_side(first, count):
        sides = []
        for n in range(first, first + count, 2):
            dense = summed(n)
            turned = pltpu.roll(dense, BS, 1)
            if n + 1 < first + count:
                second = summed(n + 1)
                top = jnp.where(left_half, dense, pltpu.roll(second, BS, 1))
                low = jnp.where(left_half, turned, second)
                side = jnp.concatenate([top, low], axis=0)
                grad_ref[n + 1] = pltpu.roll(side, BS, 1)[:, :BS]
            else:
                side = jnp.concatenate([dense, turned], axis=0)[:, :BS]
            grad_ref[n] = side[:, :BS]
            sides.append(side.astype(bf16))
        return jnp.concatenate(sides, axis=1)

    def diagonal_of(count):
        order = (count * BS, count * BS)
        return lax.broadcasted_iota(jnp.int32, order, 0) // BS == (
            lax.broadcasted_iota(jnp.int32, order, 1) // BS
        )

    clip_ref[...] = norm
    for n in range(vector_ref.shape[0]):
        vector_ref[n] = summed(owned + n)
    for (first, length), arriving, leaving in zip(spans, copies_in, copies_out):
        parts = [(n, min(4, first + length - n)) for n in range(first, first + length, 4)]
        wides = [side_by_side(*part) for part in parts]
        tall = [
            jnp.where(diagonal_of(count), jnp.concatenate([wide] * count, axis=0), 0.0)
            for (_, count), wide in zip(parts, wides)
        ]
        lefts = [product_nt(one, wide) for one, wide in zip(tall, wides)]
        rights = [product_tn(wide, wide) for wide in wides]
        for copy in arriving:
            copy.wait()
        stepped = []
        for (start, count), wide in zip(parts, wides):
            roots = left_root_ref[pl.ds(start, count)].reshape(count * BS, BS).astype(bf16)
            stepped.append(product(roots, wide))
        for (start, count), left, right in zip(parts, lefts, rights):
            here = pl.ds(start, count)
            left_ref[here] = 0.5 * left_stat_ref[here] + 0.5 * left.reshape(count, BS, BS)
            for n in range(count):
                at = n // 2 * 128
                block = right[n * BS : n * BS + BS, at : min(at + 128, count * BS)]
                if n % 2:
                    block = pltpu.roll(block, BS, 1)
                right_ref[start + n] = 0.5 * right_stat_ref[start + n] + 0.5 * block[:, :BS]
        for (start, count), value in zip(parts, stepped):
            here = pl.ds(start, count)
            value = jnp.where(diagonal_of(count), value, 0.0).astype(bf16)
            roots = right_root_ref[here].reshape(count * BS, BS).astype(bf16)
            value = product(value, roots).reshape(count, BS, BS)
            new = master_ref[here] - rate_matrix * value
            new_ref[here] = new
            copy_ref[here] = new.astype(bf16)
        for copy in leaving:
            copy.start()
    for leaving in copies_out:
        for copy in leaving:
            copy.wait()


def spans_of(owned):
    spans = []
    first = 0
    while first < owned:
        length = min(8 if first == 0 else 12, owned - first)
        spans.append((first, length))
        first += length
    return spans


def update(spot, norm, quarters, extra, *stats):
    shape = stats[0].shape
    groups = len(quarters)
    types = [f32] * 4 + [bf16]
    steps = len(spans_of(shape[0]))
    return pl.pallas_call(
        functools.partial(update_kernel, shape[0], groups),
        in_specs=[SMEM] + [VMEM_BLOCK] * (groups + 1) + [HBM] * 5,
        out_specs=[HBM] * 5 + [VMEM_BLOCK] * 2,
        out_shape=[pltpu.HBM(shape, kind) for kind in types]
        + [
            pltpu.VMEM((extra, HALF, 128), f32),
            pltpu.VMEM((1, 128), f32),
        ],
        scratch_shapes=[pltpu.VMEM(shape, f32)] * 5
        + [pltpu.VMEM(shape, kind) for kind in types]
        + [
            pltpu.SemaphoreType.DMA((5 * steps,)),
            pltpu.SemaphoreType.DMA((5 * steps,)),
        ],
        compiler_params=roomy(20),
        name="update",
    )(spot, *held_in(pltpu.VMEM, norm, *quarters), *held_in(pltpu.HBM, *stats))


def share_out(pieces, axis):
    return lax.all_to_all(pieces, axis, split_axis=0, concat_axis=0, tiled=True)


def swap(piece, distance):
    count = lax.axis_size("tile")
    return lax.ppermute(piece, "tile", [(i, i ^ distance) for i in range(count)])


def on_device(
    pixels,
    buckets,
    slot_owner_table,
    out_grad,
    master,
    left_stat,
    right_stat,
    left_root,
    right_root,
    vectors,
    moment,
):
    tile_count = lax.axis_size("tile")
    tile_place = lax.axis_index("tile")
    slot_count = pixels.shape[2]
    group_count = tile_count // STRIPS
    pairs = group_count // 2
    owned = master.shape[0]
    slots = owned * tile_count
    batch_count = lax.axis_size("batch")
    spot = lax.axis_index("batch").astype(jnp.int32).reshape(1)
    extra = extra_of(owned, batch_count)
    place = tile_place.astype(jnp.int32).reshape(1)
    paired = tile_count == 8
    if paired:
        own, for_x, for_y, for_both = pack_pieces(
            place, master, pixels[0, 0].transpose(1, 2, 0, 3)
        )
        from_x, from_y, strips_both = swap(for_x, 2), swap(for_y, 4), swap(for_both, 6)
        near_half = (owned + 1) // 2
        middle = STRIP_ROWS + near_half * HALF
        first_half = swap(from_x[STRIP_ROWS:middle], 4)
        second_half = swap(from_y[middle : STRIP_ROWS + owned * HALF], 2)
        mine = [own, from_x, from_y, strips_both, first_half, second_half]
        both = mine + [swap(piece, 1) for piece in mine]
        strips = both[:4] + both[6:10]
        pieces = [both[n] for n in (0, 1, 2, 4, 5, 6, 7, 8, 10, 11)]
        spans = [(STRIP_ROWS, owned)] * 3 + [(0, near_half), (0, owned - near_half)]
        spans = spans * 2
    else:
        pieces = [lax.all_gather(pack(master), "tile", axis=0, tiled=True).reshape(-1, 2 * BS)]
        spans = [(0, slots)]
        strips = share_out(pixels.reshape(tile_count, STRIP, C2), "tile")
        strips = [jnp.pad(strips, ((0, 0), (0, STRIP_ROWS - STRIP), (0, 0)))]

    numbers = jnp.arange(slots, dtype=jnp.int32)
    slot_of = jnp.sum(
        jnp.where(slot_owner_table[None, :] == numbers[:, None], numbers[None, :], 0), axis=1
    )
    owner = slot_of // owned
    within = slot_of - owner * owned
    place_of = slot_of
    if paired:
        apart = owner ^ tile_place
        apart = (apart & 1) * (tile_count // 2) + (apart >> 1)
        slot_of = place_of = within + owned * apart
    half = slots // 2
    near_place = jnp.where(place_of < half, place_of, half)
    far_place = jnp.where(place_of < half, half, place_of - half)
    image_ids = lax.dynamic_index_in_dim(
        buckets.reshape(group_count, slot_count), tile_place, 1, keepdims=False
    )
    turned = image_ids >= 2
    heights = jnp.where(image_ids == 0, 5 * CH // 9, jnp.where(image_ids == 1, 7 * CH // 9, CH))
    breadths = jnp.where(image_ids == 0, CW, jnp.where(image_ids == 1, 7 * CW // 9, 5 * CW // 9))
    sizes = jnp.stack(
        [
            jnp.where(turned, breadths, heights),
            jnp.where(turned, heights, breadths),
            turned,
        ],
        axis=1,
    )
    sizes = sizes.reshape(-1).astype(jnp.int32)

    two = 6 * C2 + HID2 + C2
    vec_two = jnp.concatenate([vectors[: 6 * C2], vectors[6 * C2 + HID2 : two]]).reshape(7, C2)
    vec_hid_two = vectors[6 * C2 : 6 * C2 + HID2].reshape(1, HID2)
    wide_end = two + 7 * C3
    vec_three = jnp.concatenate([vectors[two:wide_end], vectors[wide_end + HID3 :]])
    vec_three = jnp.pad(vec_three.reshape(8, C3), ((0, 0), (0, WIDE - C3)))
    vec_hid_three = vectors[wide_end : wide_end + HID3].reshape(1, HID3)

    flips = turned.reshape(-1, 1, 1, 1)
    goal = out_grad.reshape(2 * pairs, H3, W3, C3)
    goal = jnp.where(flips, goal.transpose(0, 2, 1, 3), goal)[:, :LINES]
    goal = goal.reshape(pairs, 2, LINES, W3, C3).transpose(0, 2, 3, 1, 4)
    goal = goal.reshape(pairs, LINES, 2 * W3, C3)
    goal = jnp.pad(goal, ((0, 0), (0, 0), (0, LINE - 2 * W3), (0, WIDE - C3)))
    goal = goal.reshape(pairs, AREA, WIDE)

    weights = run_unpack(slot_of, pieces, spans)
    state = run_entry(place, sizes, strips, vec_two, tile_count)
    result, *back, near, far, flat = run_main(
        (near_place, far_place),
        sizes,
        state,
        goal,
        (vec_two, vec_hid_two, vec_three, vec_hid_three),
        weights,
        tile_count,
    )
    pixel_back, vector = run_exit(sizes, state, back, flat, vec_two, tile_count)
    if paired:
        own, *parts = fold_pair(near, swap(far, 1), tile_count // 2)
        pieces = [own] + [swap(part, 2 * k + 2) for k, part in enumerate(parts)]
        vector, _ = lax.optimization_barrier((vector, parts[0]))
        vector = vector + swap(vector, 1)
        vectors_in = [vector] + [swap(vector, 2 * k) for k in range(1, tile_count // 2)]
    else:
        outgoing = jnp.concatenate([near[:half], far[:half]], axis=0)
        pieces = list(share_out(outgoing.reshape(tile_count, owned, HALF, 128), "tile"))
        vectors_in = list(lax.all_gather(vector, "tile"))
    result, pieces[1] = lax.optimization_barrier((result, pieces[1]))
    result = result.reshape(pairs, LINES, LINE, WIDE)[:, :, : 2 * W3, :C3]
    result = result.reshape(pairs, LINES, W3, 2, C3).transpose(0, 3, 1, 2, 4)
    result = result.reshape(2 * pairs, LINES, W3, C3)
    result = jnp.pad(result, ((0, 0), (0, H3 - LINES), (0, 0), (0, 0)))
    result = jnp.where(flips, result.transpose(0, 2, 1, 3), result)
    result = result.reshape(out_grad.shape)
    result = with_layout_constraint(result, Layout(major_to_minor=(0, 1, 2, 4, 5, 3, 6)))
    result, vectors_in[0] = lax.optimization_barrier((result, vectors_in[0]))
    own, *parts = fold_tile(spot, pieces, vectors_in, extra, batch_count)
    pixel_back, parts[0] = lax.optimization_barrier((pixel_back, parts[0]))
    returned = share_out(pixel_back, "tile")
    parts = [
        lax.ppermute(part, "batch", [(i, (i + k + 1) % batch_count) for i in range(batch_count)])
        for k, part in enumerate(parts)
    ]
    quarter, norm = fold_batch(spot, [own] + parts, owned, tile_count)
    returned, norm = lax.optimization_barrier((returned, norm))
    norm = share_out(norm, ("batch", "tile"))
    returned = returned.astype(f32).reshape(pixels.shape)
    returned = with_layout_constraint(returned, Layout(major_to_minor=(0, 1, 3, 4, 2, 5)))
    returned, quarter = lax.optimization_barrier((returned, quarter))
    quarters = [quarter] + [
        lax.ppermute(quarter, "batch", [(i, (i + k) % batch_count) for i in range(batch_count)])
        for k in range(1, batch_count)
    ]
    block_grad, left_new, right_new, master_new, weight_copy, whole_vector, clip = update(
        spot, norm, quarters, extra, master, left_stat, right_stat, left_root, right_root
    )
    clip_norm = clip[0, 0]
    share = vectors.shape[0] // tile_count
    whole_vector = whole_vector.reshape(-1)
    vec_grad = lax.dynamic_slice_in_dim(whole_vector, tile_place * share, share, 0)
    vec_moment = moment + vec_grad * vec_grad
    own_vectors = lax.dynamic_slice_in_dim(vectors, tile_place * share, share, 0)
    vec_new = own_vectors - rate_vector * vec_grad / (jnp.sqrt(vec_moment) + eps_adagrad)
    return (
        result,
        returned,
        clip_norm,
        block_grad,
        left_new,
        right_new,
        master_new,
        weight_copy,
        vec_grad,
        vec_moment,
        vec_new,
    )


def solution(mesh):
    placed = (
        P("batch", "tile", None, None, None, None),
        P("batch"),
        P(),
        P("batch", "tile", None, None, None, None, None),
        P("tile", None, None),
        P("tile", None, None),
        P("tile", None, None),
        P("tile", None, None),
        P("tile", None, None),
        P(),
        P("tile"),
    )
    return jax.shard_map(
        on_device,
        mesh=mesh,
        in_specs=placed,
        out_specs=(
            P("batch", "tile", None, None, None, None, None),
            P("batch", "tile", None, None, None, None),
            P(),
            P("tile", None, None),
            P("tile", None, None),
            P("tile", None, None),
            P("tile", None, None),
            P("tile", None, None),
            P("tile"),
            P("tile"),
            P("tile"),
        ),
        check_vma=False,
    )
```

```python
import functools

import jax
import jax.numpy as jnp
from jax import lax
from jax.experimental import pallas as pl
from jax.experimental.layout import Layout, with_layout_constraint
from jax.experimental.pallas import tpu as pltpu
from jax.sharding import PartitionSpec as P

C2 = 128
HID2 = 512
C3 = 320
HID3 = 1280
CH = 36
CW = 36
STRIPS = 4
BS = 64
SR = CH // STRIPS
H3 = CH // 2
W3 = CW // 2
LONG = 7 * CH // 9
LINES = LONG // 2
WIDE = 384
LINE = 40
AREA = LINES * LINE
STEP = 2 * LINE
STEPS = AREA // STEP
HALF = BS // 2
STRIP = SR * CW
STRIP_ROWS = STRIP + -STRIP % 16

eps_norm = 1e-05
clip_limit = 1.0
rate_matrix = 0.3
rate_vector = 0.3
eps_adagrad = 1e-08
f32 = jnp.float32
bf16 = jnp.bfloat16

SHAPES = [(C2, HID2), (HID2, C2), (9 * C2, C3), (C3, HID3), (HID3, C3)]
USED = sum(rows // BS * (cols // BS) for rows, cols in SHAPES)
VEC_ROWS = (6 * C2 + HID2 + C2 + C3 + 6 * C3 + HID3 + C3) // 128


VEC_BLOCKS = -(-VEC_ROWS // HALF)


def extra_of(owned, groups):
    return VEC_BLOCKS + -(owned + VEC_BLOCKS) % groups


def product(left, right):
    return jnp.dot(left, right, preferred_element_type=f32)


def product_nt(left, right):
    return lax.dot_general(left, right, (((1,), (1,)), ((), ())), preferred_element_type=f32)


def product_tn(left, right):
    return lax.dot_general(left, right, (((0,), (0,)), ((), ())), preferred_element_type=f32)


def gelu_pair(values):
    bell = jnp.exp2(values * values * (-0.5 * 1.4426950408889634))
    step = pl.reciprocal(1.0 + (0.3275911 * 0.7071067811865476) * jnp.abs(values), approx=True)
    tail = step * (
        0.5 * 0.254829592
        + step
        * (
            0.5 * -0.284496736
            + step
            * (0.5 * 1.421413741 + step * (0.5 * -1.453152027 + step * (0.5 * 1.061405429)))
        )
    )
    tail = tail * bell
    share = jnp.where(values >= 0.0, 1.0 - tail, tail)
    return (values * share, share + values * (bell * 0.3989422804014327))


def fold(values):
    chans = values.shape[-1]
    return jnp.sum(values.reshape(-1, 8, chans), axis=0)


def by_image(total):
    total = total + pltpu.roll(total, 4, 0)
    total = total + pltpu.roll(total, 2, 0)
    return jnp.sum(total, axis=1, keepdims=True)


def line(pattern):
    return jnp.concatenate([pattern] * (LINE // 8), axis=0)


def spread(pattern, chans):
    return jnp.broadcast_to(pattern, (8, chans))


def affine(values, factor, shift):
    tiles = values.reshape(-1, 8, values.shape[-1])
    return (tiles * factor + shift).reshape(values.shape)


def scaled(values, factor):
    tiles = values.reshape(-1, 8, values.shape[-1])
    return (tiles * factor).reshape(values.shape)


def from_left(values):
    return pltpu.roll(values, 2, 0)


def from_right(values):
    return pltpu.roll(values, values.shape[0] - 2, 0)


def rounded(values):
    return values.astype(bf16).astype(f32)


def widen(values):
    return jnp.concatenate([values] * (WIDE // 128), axis=-1)


def norm_terms(total, square, count):
    mean = by_image(total) / count
    scaling = lax.rsqrt(by_image(square) / count - mean * mean + eps_norm)
    return (mean, scaling)


def sweep(visit, start):
    return lax.fori_loop(0, STEPS, visit, start, unroll=True)


def step_rows(k, lines=0):
    start = k * STEP + lines * LINE
    return pl.ds(start if isinstance(k, int) else pl.multiple_of(start, LINE), STEP)


def held_in(space, *arrays):
    return [pltpu.with_memory_space_constraint(array, space) for array in arrays]


VMEM_BLOCK = pl.BlockSpec(memory_space=pltpu.VMEM)
HBM = pl.BlockSpec(memory_space=pltpu.HBM)
SMEM = pl.BlockSpec(memory_space=pltpu.SMEM)


def roomy(mebibytes):
    return pltpu.CompilerParams(vmem_limit_bytes=mebibytes * 1024 * 1024)


def image_shape(bucket_of, pair, image):
    bucket = bucket_of(2 * pair + image)
    plain = jnp.where(bucket == 0, 5 * CH // 9, 7 * CH // 9)
    across = jnp.where(bucket == 0, CW, 7 * CW // 9)
    turned = (bucket >= 2).astype(jnp.int32)
    return (
        jnp.where(turned > 0, 5 * CW // 9, plain),
        jnp.where(turned > 0, CH, across),
        turned,
    )


def bucket_reader(place_ref, bucket_ref, strip_count):
    return lambda group: bucket_ref[group * strip_count + place_ref[0]]


class Geometry:
    def __init__(self, bucket_of, pair):
        parity = lax.broadcasted_iota(jnp.int32, (8, 128), 0) % 2
        even, odd = (image_shape(bucket_of, pair, image) for image in range(2))
        high, broad, turned = (jnp.where(parity == 0, a, b) for a, b in zip(even, odd))
        self.high = high
        self.count_two = (high * broad * C2).astype(f32)[:, :1]
        self.high3 = (high + 1) // 2
        broad3 = (broad + 1) // 2
        self.count_three = (self.high3 * broad3 * C3).astype(f32)[:, :1]
        place = lax.broadcasted_iota(jnp.int32, (LINE, 128), 0) // 2
        inside = lax.broadcasted_iota(jnp.int32, (LINE, 128), 0) < 2 * W3
        self.reach = []
        self.col_share = []
        for pc in range(2):
            column = 2 * place + pc
            self.reach.append(jnp.where(inside & (column < line(broad)), line(high), 0))
            edge = (column == 0) | (column == line(broad) - 1)
            self.col_share.append(jnp.where(edge, 0.5, 1.0 / 3.0))
        self.reach3 = jnp.where(inside & (place < line(broad3)), line(self.high3), 0)
        edge3 = (place == 0) | (place == line(broad3) - 1)
        self.col_share3 = jnp.where(edge3, 0.5, 1.0 / 3.0)
        self.flipped = jnp.concatenate([turned] * (STEP // 8), axis=0) > 0

    def share(self, plane, k):
        pr, pc = plane // 2, plane % 2
        return self.lines(4 * k + pr, 2, self.reach[pc], self.col_share[pc], self.high)

    def share3(self, k):
        return self.lines(2 * k, 1, self.reach3, self.col_share3, self.high3)

    def lines(self, row, stride, reach, col_share, height):
        parts = []
        for n in range(2):
            here = row + stride * n
            row_share = jnp.where((here == 0) | (here == height - 1), 0.5, 1.0 / 3.0)
            parts.append(jnp.where(here < reach, line(row_share) * col_share, 0.0))
        return jnp.concatenate(parts, axis=0)


def strip_place(pair, spot, strip_count):
    return lax.rem(pair * 8 + strip_count - 2 + spot, strip_count)


def each_image(bucket_of, pair, visit):
    for image in range(2):
        way = image_shape(bucket_of, pair, image)[2]

        @pl.when(way == 0)
        def _():
            def one(r, carry):
                for plane in range(4):
                    row = 2 * r + plane // 2
                    strip = row // SR
                    there = pl.ds((row - strip * SR) * CW + plane % 2, W3, stride=2)
                    here = pl.ds(r * LINE + image, W3, stride=2)
                    visit(plane, here, image * STRIPS + strip, there)
                return carry

            lax.fori_loop(0, LINES, one, 0)

        @pl.when(way == 1)
        def _():
            def one(r, carry):
                for plane in range(4):
                    for strip in range(STRIPS):
                        first = (plane % 2 + strip * SR) % 2
                        count = (SR - first + 1) // 2
                        done = (strip * SR + first) // 2
                        column = 2 * r + plane // 2
                        there = pl.ds(first * CW + column, count, stride=2 * CW)
                        here = pl.ds(r * LINE + image + 2 * done, count, stride=2)
                        visit(plane, here, image * STRIPS + strip, there)
                return carry

            lax.fori_loop(0, LINES, one, 0)


def row_windows(col_ref, pc, k):
    both = col_ref[pc, step_rows(k, 1)] + col_ref[2 + pc, step_rows(k, 1)]
    return (both + col_ref[2 + pc, step_rows(k)], both + col_ref[pc, step_rows(k, 2)])


def put_col_windows(col_ref, pr, k, even, odd):
    both = even + odd
    col_ref[pr * 2, step_rows(k, 1)] = both + from_left(odd)
    col_ref[pr * 2 + 1, step_rows(k, 1)] = both + from_right(even)


def clear_edges(col_ref):
    zero_line = jnp.zeros((LINE, C2), f32)
    for plane in range(4):
        col_ref[plane, 0:LINE] = zero_line
        col_ref[plane, AREA + LINE : AREA + 2 * LINE] = zero_line


def entry_kernel(pairs, strip_count, piece_count, place_ref, bucket_ref, vec_ref, *refs):
    piece_refs, refs = refs[:piece_count], refs[piece_count:]
    x_out, inv_out, pool_out, mix_out, stat_out, image_ref, col_ref = refs
    pair = pl.program_id(0) if pairs > 1 else 0
    x_ref, inv_ref, pool_ref, mix_ref = (ref.at[0] for ref in (x_out, inv_out, pool_out, mix_out))
    bucket_of = bucket_reader(place_ref, bucket_ref, strip_count)
    shape = Geometry(bucket_of, pair)
    gain1, bias1, scale1 = (vec_ref[n : n + 1] for n in range(3))
    clear_edges(col_ref)
    if piece_count > 1:
        half = piece_count // 2
        for n, ref in enumerate(piece_refs):
            source = place_ref[0] ^ (n // half + 2 * (n % half))
            spot = lax.rem(source + 2, 2 * STRIPS)
            first = 0 if n < half else ref.shape[0] - STRIP_ROWS
            image_ref[spot] = ref[first : first + STRIP_ROWS].astype(f32)
    else:
        for spot in range(2 * STRIPS):
            source = strip_place(pair, spot, strip_count)
            image_ref[spot] = piece_refs[0][source].astype(f32)

    def take_in(plane, here, spot, there):
        x_ref[plane, here] = image_ref[spot, there]

    each_image(bucket_of, pair, take_in)

    def arrange(k, carry):
        total, square = carry
        rows = step_rows(k)
        for plane in range(4):
            share = shape.share(plane, k)
            inv_ref[plane, rows] = share
            values = jnp.where(share > 0.0, x_ref[plane, rows], 0.0)
            x_ref[plane, rows] = values
            total = total + fold(values)
            square = square + fold(values * values)
        return (total, square)

    nothing = jnp.zeros((8, C2), f32)
    total, square = sweep(arrange, (nothing, nothing))
    mean1, scaling1 = norm_terms(total, square, shape.count_two)
    factor1 = scaling1 * gain1
    shift1 = bias1 - mean1 * scaling1 * gain1

    def window_cols(k, carry):
        rows = step_rows(k)
        for pr in range(2):
            masked = []
            for pc in range(2):
                plane = pr * 2 + pc
                normal = rounded(affine(x_ref[plane, rows], factor1, shift1))
                masked.append(jnp.where(inv_ref[plane, rows] > 0.0, normal, 0.0))
            put_col_windows(col_ref, pr, k, *masked)
        return carry

    sweep(window_cols, 0)

    def mix(k, carry):
        total, square = carry
        rows = step_rows(k)
        for pc in range(2):
            windows = row_windows(col_ref, pc, k)
            for pr in range(2):
                plane = pr * 2 + pc
                values = x_ref[plane, rows]
                share = inv_ref[plane, rows]
                pooled = windows[pr] * share - rounded(affine(values, factor1, shift1))
                pooled = jnp.where(share > 0.0, pooled, 0.0)
                mixed = values + scale1 * pooled
                pool_ref[plane, rows] = pooled
                mix_ref[plane, rows] = mixed
                total = total + fold(mixed)
                square = square + fold(mixed * mixed)
        return (total, square)

    total, square = sweep(mix, (nothing, nothing))
    mean2, scaling2 = norm_terms(total, square, shape.count_two)
    for n, value in enumerate((mean1, scaling1, mean2, scaling2)):
        stat_out[0, n] = spread(value, 128)


def pair_specs(pairs, shapes, mode=None):
    if pairs == 1:
        return [VMEM_BLOCK] * len(shapes)
    return [
        pl.BlockSpec(
            (1,) + shape, lambda t, rank=len(shape): (t,) + (0,) * rank, pipeline_mode=mode
        )
        for shape in shapes
    ]


def whole_specs(pairs, shapes):
    if pairs == 1:
        return [VMEM_BLOCK] * len(shapes)
    return [
        pl.BlockSpec(
            shape,
            lambda t, rank=len(shape): (0,) * rank,
            pipeline_mode=pl.Buffered(1),
        )
        for shape in shapes
    ]


def pair_arrays(pairs, shapes, kinds):
    make = pltpu.VMEM if pairs == 1 else jax.ShapeDtypeStruct
    return [make((pairs,) + shape, kind) for shape, kind in zip(shapes, kinds)]


STATE = [(4, AREA, C2)] * 4 + [(4, 8, 128)]
BACK = [(4, AREA, C2)] * 2 + [(2, 8, 128)]


def run_entry(place, buckets, pieces, vec, strip_count):
    pairs = strip_count // 8
    if pairs == 1:
        pieces = held_in(pltpu.VMEM, *pieces)
    return pl.pallas_call(
        functools.partial(entry_kernel, pairs, strip_count, len(pieces)),
        grid=() if pairs == 1 else (pairs,),
        in_specs=[SMEM] * 2 + whole_specs(pairs, [array.shape for array in (vec, *pieces)]),
        out_specs=pair_specs(pairs, STATE),
        out_shape=pair_arrays(pairs, STATE, [f32] * 5),
        scratch_shapes=[
            pltpu.VMEM((2 * STRIPS, STRIP_ROWS, C2), f32),
            pltpu.VMEM((4, AREA + 2 * LINE, C2), f32),
        ],
        compiler_params=roomy(6 if pairs == 1 else 40),
        name="entry",
    )(place, buckets, vec, *pieces)


WEIGHTS = [(C2, HID2), (HID2, C2), (9 * C2, WIDE), (WIDE, HID3), (HID3, WIDE)]


def unpack_kernel(spans, slot_ref, *refs):
    piece_refs, refs = refs[: len(spans)], refs[len(spans) :]
    weights, gathered_ref = refs[:-1], refs[-1]
    done = 0
    for ref, (first, count) in zip(piece_refs, spans):
        blocks = ref[first : first + count * HALF].reshape(count, HALF, 128)
        gathered_ref[done : done + count] = blocks
        done += count
    left_half = lax.broadcasted_iota(jnp.int32, (HALF, 128), 1) < BS
    offset = 0
    for (rows, cols), ref in zip(SHAPES, weights):
        wide = cols // BS
        for rb in range(rows // BS):
            for cb in range(0, wide, 2):
                number = offset + rb * wide + cb
                first = gathered_ref[slot_ref[number]]
                turned = pltpu.roll(first, BS, 1)
                if cb + 1 < wide:
                    second = gathered_ref[slot_ref[number + 1]]
                    top = jnp.where(left_half, first, pltpu.roll(second, BS, 1))
                    low = jnp.where(left_half, turned, second)
                else:
                    top = jnp.where(left_half, first, 0.0)
                    low = jnp.where(left_half, turned, 0.0)
                place = slice(cb * BS, cb * BS + 128)
                ref[rb * BS : rb * BS + HALF, place] = top
                ref[rb * BS + HALF : rb * BS + BS, place] = low
        offset += rows // BS * wide
    weights[3][C3:, :] = jnp.zeros((WIDE - C3, HID3), bf16)


def run_unpack(slot_of, pieces, spans):
    slots = slot_of.shape[0]
    return pl.pallas_call(
        functools.partial(unpack_kernel, spans),
        in_specs=[SMEM] + [VMEM_BLOCK] * len(pieces),
        out_specs=[VMEM_BLOCK] * 5,
        out_shape=[pltpu.VMEM(shape, bf16) for shape in WEIGHTS],
        scratch_shapes=[pltpu.VMEM((slots, HALF, 128), bf16)],
        compiler_params=roomy(6),
        name="unpack",
    )(slot_of, *held_in(pltpu.VMEM, *pieces))


def main_kernel(
    pairs,
    strip_count,
    slots,
    near_place,
    far_place,
    place_ref,
    bucket_ref,
    inv_in,
    mix_in,
    stat_in,
    goal_ref,
    vec_ref,
    w1_ref,
    w2_ref,
    we_ref,
    w3_ref,
    w4_ref,
    result_ref,
    zed_out,
    dx_out,
    mean_out,
    near_ref,
    far_ref,
    flat_ref,
    zed_ref,
    hid_ref,
    u_ref,
    g_ref,
    h_ref,
    dy_ref,
    patch_ref,
    dpatch_ref,
    inv3_ref,
    e_ref,
    col3_ref,
    pool3_ref,
    mix3_ref,
    dx3_ref,
    hid3_ref,
    dhid3_ref,
    u3_ref,
    g3_ref,
    h3_ref,
    dy3_ref,
    dpre_ref,
    gw1_ref,
    gw2_ref,
    gwe_ref,
    gw3_ref,
    gw4_ref,
    acc_two,
    acc_hid_two,
    acc_three,
    acc_hid_three,
):
    pair = pl.program_id(0) if pairs > 1 else 0
    grads = [gw1_ref, gw2_ref, gwe_ref, gw3_ref, gw4_ref]
    inv_ref, mix_ref, stat_ref = (ref.at[0] for ref in (inv_in, mix_in, stat_in))
    back_ref, dx_ref = zed_out.at[0], dx_out.at[0]
    left_half = lax.broadcasted_iota(jnp.int32, (HALF, 128), 1) < BS

    def at_pair(number, act):
        if pairs == 1:
            act()
        else:
            pl.when(pair == number)(act)

    def begin():
        acc_two[...] = jnp.zeros(acc_two.shape, f32)
        acc_hid_two[...] = jnp.zeros(acc_hid_two.shape, f32)
        acc_three[...] = jnp.zeros(acc_three.shape, f32)
        acc_hid_three[...] = jnp.zeros(acc_hid_three.shape, f32)

    at_pair(0, begin)
    shape = Geometry(bucket_reader(place_ref, bucket_ref, strip_count), pair)
    count_two, count_three, flipped = shape.count_two, shape.count_three, shape.flipped
    nothing = jnp.zeros((8, C2), f32)
    nothing3 = jnp.zeros((8, WIDE), f32)

    def vector_row(at, length):
        first, shift = at // 128, at % 128
        count = -(-(shift + length) // 128)
        row = jnp.concatenate([vec_ref[first + n : first + n + 1] for n in range(count)], axis=1)
        if shift:
            row = pltpu.roll(jnp.broadcast_to(row, (8, count * 128)), count * 128 - shift, 1)[:1]
        return row

    def wide_row(at):
        lane = lax.broadcasted_iota(jnp.int32, (1, WIDE), 1)
        return jnp.where(lane < C3, vector_row(at, C3)[:, :WIDE], 0.0)

    gain2, bias2, scale2 = (vec_ref[n : n + 1] for n in range(3, 6))
    hid_bias = vector_row(6 * C2, HID2)
    out_bias = vector_row(6 * C2 + HID2, C2)
    two = 7 * C2 + HID2
    embed_bias, gain3, bias3, scale3 = (wide_row(two + n * C3) for n in range(4))
    gain4, bias4, scale4 = (wide_row(two + n * C3) for n in range(4, 7))
    hid_bias3 = vector_row(two + 7 * C3, HID3)[:, :HID3]
    out_bias3 = wide_row(two + 7 * C3 + HID3)
    mean2, scaling2 = stat_ref[2], stat_ref[3]
    factor2 = scaling2 * gain2
    shift2 = bias2 - mean2 * scaling2 * gain2
    for plane in range(4):
        zed_ref[plane, 0:LINE] = jnp.zeros((LINE, C2), f32)
    col3_ref[0:LINE] = jnp.zeros((LINE, WIDE), f32)
    col3_ref[AREA + LINE : AREA + 2 * LINE] = jnp.zeros((LINE, WIDE), f32)

    def put_block(number, block):
        near_ref[near_place[number]] = block
        far_ref[far_place[number]] = block

    def pack_blocks(matrices):
        offsets = [0]
        for rows, cols in SHAPES:
            offsets.append(offsets[-1] + rows // BS * (cols // BS))
        for which in matrices:
            (rows, cols), ref = SHAPES[which], grads[which]
            wide = cols // BS
            for rb in range(rows // BS):
                for cb in range(0, wide, 2):
                    number = offsets[which] + rb * wide + cb
                    at = slice(cb * BS, cb * BS + 128)
                    top = ref[rb * BS : rb * BS + HALF, at].astype(bf16)
                    low = ref[rb * BS + HALF : rb * BS + BS, at].astype(bf16)
                    put_block(number, jnp.where(left_half, top, pltpu.roll(low, BS, 1)))
                    if cb + 1 < wide:
                        put_block(number + 1, jnp.where(left_half, pltpu.roll(top, BS, 1), low))

    def plane_rows(plane):
        return slice(plane * AREA, plane * AREA + AREA)

    def begin_plane(plane):
        low = affine(mix_ref[plane], factor2, shift2).astype(bf16)
        h_ref[plane_rows(plane)] = low
        hid_ref[plane % 2] = product(low, w1_ref[...])

    begin_plane(0)
    for plane in range(4):
        if plane < 3:
            begin_plane(plane + 1)
        for k in range(STEPS):
            rows = step_rows(k)
            flat = slice(plane * AREA + k * STEP, plane * AREA + k * STEP + STEP)
            for at in range(0, HID2, 128):
                lanes = slice(at, at + 128)
                active, slope = gelu_pair(hid_ref[plane % 2, rows, lanes] + hid_bias[:, lanes])
                u_ref[flat, lanes] = active.astype(bf16)
                g_ref[flat, lanes] = slope.astype(bf16)
        out = product(u_ref[plane_rows(plane)], w2_ref[...]) + out_bias
        zed = jnp.where(inv_ref[plane] > 0.0, mix_ref[plane] + scale2 * out, 0.0)
        zed_ref[plane, LINE : LINE + AREA] = rounded(zed)

    def patches(k, carry):
        rows = step_rows(k)
        taps = []
        for ky in range(3):
            pr = (0 if ky == 1 else 1) * 2
            source = step_rows(k, 0 if ky == 0 else 1)
            even = zed_ref[pr, source]
            odd = zed_ref[pr + 1, source]
            taps.append((from_left(odd), even, odd))
        for ky in range(3):
            for kx in range(3):
                at = (3 * ky + kx) * C2
                tap = taps[ky][kx]
                if ky != kx:
                    tap = jnp.where(flipped, taps[kx][ky], tap)
                patch_ref[rows, at : at + C2] = tap.astype(bf16)
        return carry

    sweep(patches, 0)
    e_ref[...] = product(patch_ref[...], we_ref[...])

    def embed(k, carry):
        total, square = carry
        rows = step_rows(k)
        share = shape.share3(k)
        inv3_ref[rows] = share
        out = jnp.where(widen(share) > 0.0, e_ref[rows] + embed_bias, 0.0)
        e_ref[rows] = out
        return (total + fold(out), square + fold(out * out))

    total, square = sweep(embed, (nothing3, nothing3))
    mean3, scaling3 = norm_terms(total, square, count_three)
    factor3 = scaling3 * gain3
    shift3 = bias3 - mean3 * scaling3 * gain3

    def window_cols3(k, carry):
        rows = step_rows(k)
        normal = rounded(affine(e_ref[rows], factor3, shift3))
        masked = jnp.where(widen(inv3_ref[rows]) > 0.0, normal, 0.0)
        col3_ref[step_rows(k, 1)] = masked + from_left(masked) + from_right(masked)
        return carry

    sweep(window_cols3, 0)

    def row_windows3(k):
        return col3_ref[step_rows(k)] + col3_ref[step_rows(k, 1)] + col3_ref[step_rows(k, 2)]

    def mix3(k, carry):
        total, square = carry
        rows = step_rows(k)
        values = e_ref[rows]
        share = widen(inv3_ref[rows])
        pooled = row_windows3(k) * share - rounded(affine(values, factor3, shift3))
        pooled = jnp.where(share > 0.0, pooled, 0.0)
        mixed = values + scale3 * pooled
        pool3_ref[rows] = pooled
        mix3_ref[rows] = mixed
        return (total + fold(mixed), square + fold(mixed * mixed))

    total, square = sweep(mix3, (nothing3, nothing3))
    mean4, scaling4 = norm_terms(total, square, count_three)
    factor4 = scaling4 * gain4
    shift4 = bias4 - mean4 * scaling4 * gain4
    normal4 = (spread(scaling4, WIDE), spread(-mean4 * scaling4, WIDE))

    def prepare3(k, d_bias):
        rows = step_rows(k)
        h3_ref[rows] = affine(mix3_ref[rows], factor4, shift4).astype(bf16)
        goal = goal_ref[0, rows].astype(f32)
        goal = jnp.where(widen(inv3_ref[rows]) > 0.0, goal, 0.0)
        low_goal = (scale4 * goal).astype(bf16)
        dy3_ref[rows] = low_goal
        return d_bias + fold(low_goal.astype(f32))

    acc_three[7] += sweep(prepare3, nothing3)

    def keep(ref, value, place=slice(None)):
        if pairs == 1:
            ref[place] = value.astype(ref.dtype)
        else:

            @pl.when(pair == 0)
            def _():
                ref[place] = value

            @pl.when(pair > 0)
            def _():
                ref[place] += value

    def begin_chunk(at):
        lanes = slice(at, at + 256)
        hid3_ref[:, lanes] = product(h3_ref[...], w3_ref[:, lanes])
        dhid3_ref[:, lanes] = product_nt(dy3_ref[...], w4_ref[lanes])

    begin_chunk(0)
    for at in range(0, HID3, 256):
        if at + 256 < HID3:
            begin_chunk(at + 256)
        for lane in (at, at + 128):
            lanes = slice(lane, lane + 128)
            total = nothing
            for k in range(STEPS):
                rows = step_rows(k)
                active, slope = gelu_pair(hid3_ref[rows, lanes] + hid_bias3[:, lanes])
                u3_ref[rows, lanes] = active.astype(bf16)
                low = (slope * dhid3_ref[rows, lanes]).astype(bf16)
                g3_ref[rows, lanes] = low
                total = total + fold(low.astype(f32))
            acc_hid_three[:, lanes] += total
        lanes = slice(at, at + 256)
        out = product(u3_ref[:, lanes], w4_ref[lanes])
        d_low = product_nt(g3_ref[:, lanes], w3_ref[:, lanes])
        result_ref[0] = out if at == 0 else result_ref[0] + out
        dx3_ref[...] = d_low if at == 0 else dx3_ref[...] + d_low
        keep(gw3_ref, product_tn(h3_ref[...], g3_ref[:, lanes]), (slice(None), lanes))
        keep(gw4_ref, product_tn(u3_ref[:, lanes], dy3_ref[...]), lanes)

    def finish3(k, carry):
        d_scale, d_shift, d_gain = carry
        rows = step_rows(k)
        valid = widen(inv3_ref[rows]) > 0.0
        mixed = mix3_ref[rows]
        out = jnp.where(valid, result_ref[0, rows] + out_bias3, 0.0)
        result_ref[0, rows] = mixed + scale4 * out
        d_scale = d_scale + fold(out * goal_ref[0, rows].astype(f32))
        d_low = dx3_ref[rows]
        normal = affine(mixed, *normal4)
        return (d_scale, d_shift + fold(d_low), d_gain + fold(d_low * normal))

    d_scale, d_shift, d_gain = sweep(finish3, (nothing3, nothing3, nothing3))
    acc_three[6] += d_scale
    acc_three[5] += d_shift
    acc_three[4] += d_gain
    mean_shift = by_image(d_shift * gain4) / count_three
    mean_gain = by_image(d_gain * gain4) / count_three
    back_gain4 = scaling4 * gain4
    back_mean4 = spread(-scaling4 * mean_shift, WIDE)
    back_normal4 = spread(scaling4 * mean_gain, WIDE)

    def unmix3(k, d_scale):
        rows = step_rows(k)
        share = widen(inv3_ref[rows])
        valid = share > 0.0
        normal = affine(mix3_ref[rows], *normal4)
        back = affine(dx3_ref[rows], back_gain4, back_mean4) - scaled(normal, back_normal4)
        d_mixed = jnp.where(valid, back + goal_ref[0, rows].astype(f32), 0.0)
        dx3_ref[rows] = d_mixed
        d_scale = d_scale + fold(pool3_ref[rows] * d_mixed)
        weighted = scale3 * d_mixed * share
        col3_ref[step_rows(k, 1)] = weighted + from_left(weighted) + from_right(weighted)
        return d_scale

    acc_three[3] += sweep(unmix3, nothing3)
    normal3 = (spread(scaling3, WIDE), spread(-mean3 * scaling3, WIDE))

    def unpool3(k, carry):
        d_shift, d_gain = carry
        rows = step_rows(k)
        valid = widen(inv3_ref[rows]) > 0.0
        d_normal = jnp.where(valid, row_windows3(k) - scale3 * dx3_ref[rows], 0.0)
        pool3_ref[rows] = d_normal
        normal = affine(e_ref[rows], *normal3)
        return (d_shift + fold(d_normal), d_gain + fold(d_normal * normal))

    d_shift, d_gain = sweep(unpool3, (nothing3, nothing3))
    acc_three[2] += d_shift
    acc_three[1] += d_gain
    mean_shift = by_image(d_shift * gain3) / count_three
    mean_gain = by_image(d_gain * gain3) / count_three
    back_gain3 = scaling3 * gain3
    back_mean3 = spread(-scaling3 * mean_shift, WIDE)
    back_normal3 = spread(scaling3 * mean_gain, WIDE)

    def unnorm3(k, d_bias):
        rows = step_rows(k)
        valid = widen(inv3_ref[rows]) > 0.0
        normal = affine(e_ref[rows], *normal3)
        back = affine(pool3_ref[rows], back_gain3, back_mean3) - scaled(normal, back_normal3)
        low = jnp.where(valid, dx3_ref[rows] + back, 0.0).astype(bf16)
        dpre_ref[rows] = low
        return d_bias + fold(low.astype(f32))

    acc_three[0] += sweep(unnorm3, nothing3)
    keep(gwe_ref, product_tn(patch_ref[...], dpre_ref[...]))
    dpatch_ref[0:AREA] = product_nt(dpre_ref[...], we_ref[...])
    dpatch_ref[AREA : AREA + LINE] = jnp.zeros((LINE, 9 * C2), f32)

    def gather_back(k, carry):
        rows = step_rows(k)

        def tap(ky, kx, source):
            at = (3 * ky + kx) * C2
            value = dpatch_ref[source, at : at + C2]
            if ky != kx:
                at = (3 * kx + ky) * C2
                value = jnp.where(flipped, dpatch_ref[source, at : at + C2], value)
            return value

        sources = []
        for ky in range(3):
            source = step_rows(k, 1 if ky == 0 else 0)
            sources.append(
                (tap(ky, 1, source), tap(ky, 2, source) + from_right(tap(ky, 0, source)))
            )
        for pc in range(2):
            for pr, value in ((0, sources[1][pc]), (1, sources[2][pc] + sources[0][pc])):
                plane = pr * 2 + pc
                valid = inv_ref[plane, rows] > 0.0
                back_ref[plane, rows] = jnp.where(valid, rounded(value), 0.0)
        return carry

    sweep(gather_back, 0)

    if pairs == 1:
        pack_blocks(range(2, 5))

    normal2 = (spread(scaling2, C2), spread(-mean2 * scaling2, C2))

    def begin_back(plane):
        low_goal = (scale2 * back_ref[plane]).astype(bf16)
        dy_ref[plane_rows(plane)] = low_goal
        hid_ref[plane % 2] = product_nt(low_goal, w2_ref[...])
        return fold(low_goal.astype(f32))

    d_out_bias = begin_back(0)
    d_shift, d_gain = nothing, nothing
    sums = [nothing] * (HID2 // 128)
    new_gw1, new_gw2 = None, None
    for plane in range(4):
        if plane < 3:
            d_out_bias = d_out_bias + begin_back(plane + 1)
        for k in range(STEPS):
            rows = step_rows(k)
            part = slice(plane * AREA + k * STEP, plane * AREA + k * STEP + STEP)
            for n, at in enumerate(range(0, HID2, 128)):
                lanes = slice(at, at + 128)
                low = g_ref[part, lanes].astype(f32) * hid_ref[plane % 2, rows, lanes]
                low = low.astype(bf16)
                g_ref[part, lanes] = low
                sums[n] = sums[n] + fold(low.astype(f32))
        flat = plane_rows(plane)
        d_low = product_nt(g_ref[flat], w1_ref[...])
        dx_ref[plane] = d_low
        d_shift = d_shift + fold(d_low)
        d_gain = d_gain + fold(d_low * affine(mix_ref[plane], *normal2))
        part_gw1 = product_tn(h_ref[flat], g_ref[flat])
        part_gw2 = product_tn(dy_ref[flat], u_ref[flat])
        new_gw1 = part_gw1 if plane == 0 else new_gw1 + part_gw1
        new_gw2 = part_gw2 if plane == 0 else new_gw2 + part_gw2
    new_gw2 = new_gw2.T
    for n, value in enumerate(sums):
        acc_hid_two[:, n * 128 : n * 128 + 128] += value
    acc_two[6] += d_out_bias
    acc_two[4] += d_shift
    acc_two[3] += d_gain
    mean_out[0, 0] = spread(by_image(d_shift * gain2) / count_two, 128)
    mean_out[0, 1] = spread(by_image(d_gain * gain2) / count_two, 128)
    keep(gw1_ref, new_gw1)
    keep(gw2_ref, new_gw2)
    d_scale = fold(w2_ref[...].astype(f32) * new_gw2) + out_bias * d_out_bias
    acc_two[5] += d_scale / scale2

    def finish():
        if pairs > 1:
            pack_blocks(range(5))
        else:
            pack_blocks(range(2))

        def filler(number, carry):
            put_block(number, jnp.zeros((HALF, 128), bf16))
            return carry

        lax.fori_loop(USED, slots, filler, 0)

        flat_ref[...] = jnp.zeros(flat_ref.shape, f32)

        def put(at, total, length):
            if at % 128:
                room = jnp.zeros((8, 128), f32)
                if total.shape[1] < length + BS:
                    total = jnp.concatenate([total, room], axis=1)
                total = pltpu.roll(total, BS, 1)
            whole = jnp.sum(total, axis=0, keepdims=True)
            done = -(at % 128)
            row = at // 128
            lane = 0
            while done < length:
                first = max(0, -done)
                last = min(128, length - done)
                flat_ref[row : row + 1, first:last] = whole[:, lane + first : lane + last]
                done += 128
                lane += 128
                row += 1

        at = 3 * C2
        for n in range(3, 6):
            put(at, acc_two[n], C2)
            at += C2
        put(at, acc_hid_two[...], HID2)
        at += HID2
        put(at, acc_two[6], C2)
        at += C2
        for n in range(7):
            put(at, acc_three[n], C3)
            at += C3
        put(at, acc_hid_three[...], HID3)
        at += HID3
        put(at, acc_three[7], C3)

    at_pair(pairs - 1, finish)


def run_main(places, place, buckets, state, goal, vec, weights, strip_count):
    pairs = goal.shape[0]
    slots = places[0].shape[0]
    half = slots // 2 + 1
    if pairs == 1:
        state = held_in(pltpu.VMEM, *state)
    weights = held_in(pltpu.VMEM, *weights)
    _, inv, _, mix, stat = state
    state_shapes = [STATE[1], STATE[3], STATE[4]]
    grad_kind = bf16 if pairs == 1 else f32
    wide_f32 = pltpu.VMEM((AREA, WIDE), f32)
    wide_bf16 = pltpu.VMEM((AREA, WIDE), bf16)
    scratch = [
        pltpu.VMEM((4, AREA + LINE, C2), f32),
        pltpu.VMEM((2, AREA, HID2), f32),
        pltpu.VMEM((4 * AREA, HID2), bf16),
        pltpu.VMEM((4 * AREA, HID2), bf16),
        pltpu.VMEM((4 * AREA, C2), bf16),
        pltpu.VMEM((4 * AREA, C2), bf16),
        pltpu.VMEM((AREA, 9 * C2), bf16),
        pltpu.VMEM((AREA + LINE, 9 * C2), f32),
        pltpu.VMEM((AREA, 128), f32),
        wide_f32,
        pltpu.VMEM((AREA + 2 * LINE, WIDE), f32),
        wide_f32,
        wide_f32,
        wide_f32,
        pltpu.VMEM((AREA, HID3), f32),
        pltpu.VMEM((AREA, HID3), f32),
        pltpu.VMEM((AREA, HID3), bf16),
        pltpu.VMEM((AREA, HID3), bf16),
        wide_bf16,
        wide_bf16,
        wide_bf16,
        pltpu.VMEM((C2, HID2), grad_kind),
        pltpu.VMEM((HID2, C2), grad_kind),
        pltpu.VMEM((9 * C2, WIDE), grad_kind),
        pltpu.VMEM((WIDE, HID3), grad_kind),
        pltpu.VMEM((HID3, WIDE), grad_kind),
        pltpu.VMEM((7, 8, C2), f32),
        pltpu.VMEM((8, HID2), f32),
        pltpu.VMEM((8, 8, WIDE), f32),
        pltpu.VMEM((8, HID3), f32),
    ]
    out_shapes = [(half, HALF, 128), (half, HALF, 128), (VEC_BLOCKS * HALF, 128)]
    make = pltpu.VMEM if pairs == 1 else jax.ShapeDtypeStruct
    return pl.pallas_call(
        functools.partial(main_kernel, pairs, strip_count, slots),
        grid=() if pairs == 1 else (pairs,),
        in_specs=[SMEM] * 4
        + pair_specs(pairs, state_shapes + [goal.shape[1:]], pl.Buffered(1))
        + whole_specs(pairs, [vec.shape])
        + [VMEM_BLOCK] * 5,
        out_specs=pair_specs(pairs, [(AREA, WIDE)] + BACK) + whole_specs(pairs, out_shapes),
        out_shape=pair_arrays(pairs, [(AREA, WIDE)] + BACK, [f32] * 4)
        + [make(shape, kind) for shape, kind in zip(out_shapes, (bf16, bf16, f32))],
        scratch_shapes=scratch,
        compiler_params=pltpu.CompilerParams(
            vmem_limit_bytes=(40 if pairs == 1 else 56) * 1024 * 1024,
            fuse_transposed_lhs_in_matmul=True,
        ),
        name="blocks",
    )(*places, place, buckets, inv, mix, stat, goal, vec, *weights)


def exit_kernel(
    pairs,
    strip_count,
    place_ref,
    bucket_ref,
    x_in,
    inv_in,
    pool_in,
    mix_in,
    stat_in,
    zed_in,
    dx_in,
    mean_in,
    flat_ref,
    vec_ref,
    payload_hbm,
    vector_ref,
    payload_ref,
    image_ref,
    col_ref,
    dx_ref,
    back_ref,
    acc_ref,
    sem,
):
    pair = pl.program_id(0) if pairs > 1 else 0
    x_ref, inv_ref, pool_ref, mix_ref, stat_ref, zed_ref, low_ref, mean_ref = (
        ref.at[0] for ref in (x_in, inv_in, pool_in, mix_in, stat_in, zed_in, dx_in, mean_in)
    )
    bucket_of = bucket_reader(place_ref, bucket_ref, strip_count)
    shape = Geometry(bucket_of, pair)
    count_two = shape.count_two
    gain1, bias1, scale1, gain2 = (vec_ref[n : n + 1] for n in range(4))
    mean1, scaling1, mean2, scaling2 = (stat_ref[n] for n in range(4))
    normal2 = (scaling2, -mean2 * scaling2)
    clear_edges(col_ref)
    nothing = jnp.zeros((8, C2), f32)
    back_gain2 = scaling2 * gain2
    back_mean2 = -scaling2 * mean_ref[0]
    back_normal2 = scaling2 * mean_ref[1]

    if pairs > 1:

        @pl.when(pair == 0)
        def _():
            acc_ref[...] = jnp.zeros(acc_ref.shape, f32)

    def add_up(n, total):
        acc_ref[n] = total if pairs == 1 else acc_ref[n] + total

    def unmix(k, d_scale):
        rows = step_rows(k)
        for pr in range(2):
            weighted = []
            for pc in range(2):
                plane = pr * 2 + pc
                share = inv_ref[plane, rows]
                normal = affine(mix_ref[plane, rows], *normal2)
                back = affine(low_ref[plane, rows], back_gain2, back_mean2)
                back = back - scaled(normal, back_normal2)
                d_mixed = jnp.where(share > 0.0, zed_ref[plane, rows] + back, 0.0)
                dx_ref[plane, rows] = d_mixed
                d_scale = d_scale + fold(pool_ref[plane, rows] * d_mixed)
                weighted.append(scale1 * d_mixed * share)
            put_col_windows(col_ref, pr, k, *weighted)
        return d_scale

    add_up(2, sweep(unmix, nothing))
    normal1 = (spread(scaling1, C2), spread(-mean1 * scaling1, C2))

    def unpool(k, carry):
        d_shift, d_gain = carry
        rows = step_rows(k)
        for pc in range(2):
            windows = row_windows(col_ref, pc, k)
            for pr in range(2):
                plane = pr * 2 + pc
                valid = inv_ref[plane, rows] > 0.0
                d_normal = windows[pr] - scale1 * dx_ref[plane, rows]
                d_normal = jnp.where(valid, d_normal, 0.0)
                back_ref[plane, rows] = d_normal
                normal = affine(x_ref[plane, rows], *normal1)
                d_shift = d_shift + fold(d_normal)
                d_gain = d_gain + fold(d_normal * normal)
        return (d_shift, d_gain)

    d_shift, d_gain = sweep(unpool, (nothing, nothing))
    add_up(1, d_shift)
    add_up(0, d_gain)
    mean_shift = by_image(d_shift * gain1) / count_two
    mean_gain = by_image(d_gain * gain1) / count_two
    back_gain1 = scaling1 * gain1
    back_mean1 = spread(-scaling1 * mean_shift, C2)
    back_normal1 = spread(scaling1 * mean_gain, C2)

    def unnorm(k, carry):
        rows = step_rows(k)
        for plane in range(4):
            normal = affine(x_ref[plane, rows], *normal1)
            back = affine(back_ref[plane, rows], back_gain1, back_mean1)
            back = back - scaled(normal, back_normal1)
            valid = inv_ref[plane, rows] > 0.0
            dx_ref[plane, rows] = jnp.where(valid, dx_ref[plane, rows] + back, 0.0)
        return carry

    sweep(unnorm, 0)

    def give_back(plane, here, spot, there):
        image_ref[spot, there] = dx_ref[plane, here]

    image_ref[...] = jnp.zeros(image_ref.shape, f32)
    each_image(bucket_of, pair, give_back)

    for spot in range(2 * STRIPS):
        target = strip_place(pair, spot, strip_count)
        for within in range(SR):
            rows = slice(within * CW, within * CW + CW)
            payload_ref[target, within] = image_ref[spot, rows].astype(bf16)

    def finish():
        copy = pltpu.make_async_copy(payload_ref, payload_hbm, sem)
        copy.start()
        vector_ref[...] = flat_ref[...]
        for n in range(3):
            vector_ref[n : n + 1] = jnp.sum(acc_ref[n], axis=0, keepdims=True)
        copy.wait()

    if pairs == 1:
        finish()
    else:
        pl.when(pair == pairs - 1)(finish)


def run_exit(place, buckets, state, back, flat, vec, strip_count):
    pairs = strip_count // 8
    payload = (strip_count, SR, CW, C2)
    make = pltpu.VMEM if pairs == 1 else jax.ShapeDtypeStruct
    plane_f32 = pltpu.VMEM((4, AREA, C2), f32)
    arrays = [*state, *back]
    if pairs == 1:
        arrays = held_in(pltpu.VMEM, *arrays)
    return pl.pallas_call(
        functools.partial(exit_kernel, pairs, strip_count),
        grid=() if pairs == 1 else (pairs,),
        in_specs=[SMEM] * 2
        + pair_specs(pairs, STATE + BACK, pl.Buffered(1))
        + whole_specs(pairs, [flat.shape, vec.shape]),
        out_specs=[HBM] + whole_specs(pairs, [flat.shape]),
        out_shape=[pltpu.HBM(payload, bf16), make(flat.shape, f32)],
        scratch_shapes=[
            pltpu.VMEM(payload, bf16),
            pltpu.VMEM((2 * STRIPS, STRIP_ROWS, C2), f32),
            pltpu.VMEM((4, AREA + 2 * LINE, C2), f32),
            plane_f32,
            plane_f32,
            pltpu.VMEM((3, 8, C2), f32),
            pltpu.SemaphoreType.DMA,
        ],
        compiler_params=roomy(8 if pairs == 1 else 40),
        name="exit",
    )(place, buckets, *arrays, flat, vec)


def dense_blocks(values):
    return jnp.concatenate([values[:, :HALF], values[:, HALF:]], axis=2).astype(bf16)


def pack_kernel(master_ref, dense_ref):
    dense_ref[...] = dense_blocks(master_ref[...])


def pack(master):
    owned = master.shape[0]
    return pl.pallas_call(
        pack_kernel,
        out_shape=jax.ShapeDtypeStruct((owned, HALF, 2 * BS), bf16),
        name="pack",
    )(master)


def pack_pieces_kernel(place_ref, master_hbm, pixel_hbm, *refs):
    out_refs, (wide_ref, master_ref, pixel_ref, sem) = refs[:-4], refs[-4:]
    owned = master_ref.shape[0]
    slots = pixel_ref.shape[2]
    copies = [pltpu.make_async_copy(pixel_hbm, pixel_ref, sem.at[0])]
    parts = [(0, owned // 2), (owned // 2, owned - owned // 2)]
    for n, part in enumerate(parts):
        copies.append(
            pltpu.make_async_copy(
                master_hbm.at[pl.ds(*part)], master_ref.at[pl.ds(*part)], sem.at[1 + n]
            )
        )
    for copy in copies:
        copy.start()
    copies[0].wait()

    def widen_row(row, carry):
        start = pl.multiple_of(row * CW * slots, 8)
        values = pixel_ref[row].astype(f32).reshape(CW * slots, C2)
        wide_ref[pl.ds(start, CW * slots)] = values
        return carry

    lax.fori_loop(0, SR, widen_row, 0)
    for k, ref in enumerate(out_refs):
        for other in range(2):
            slot = place_ref[0] ^ (2 * k + other)
            first = other * (ref.shape[0] - STRIP_ROWS)
            strip = wide_ref[pl.ds(slot, STRIP_ROWS, stride=slots)]
            ref[first : first + STRIP_ROWS] = strip.astype(bf16)
    for (first, count), copy in zip(parts, copies[1:]):
        copy.wait()
        dense = dense_blocks(master_ref[first : first + count]).reshape(count * HALF, 2 * BS)
        start = STRIP_ROWS + first * HALF
        for ref in out_refs[:3]:
            ref[start : start + count * HALF] = dense


def pack_pieces(place, master, pixels):
    slots = pixels.shape[2]
    rows = master.shape[0] * HALF
    shapes = [(rows + 2 * STRIP_ROWS, 2 * BS)] * 3 + [(2 * STRIP_ROWS, 2 * BS)]
    return pl.pallas_call(
        pack_pieces_kernel,
        in_specs=[SMEM] + [HBM] * 2,
        out_specs=[VMEM_BLOCK] * 4,
        out_shape=[pltpu.VMEM(shape, bf16) for shape in shapes],
        scratch_shapes=[
            pltpu.VMEM((STRIP_ROWS * slots, C2), f32),
            pltpu.VMEM(master.shape, f32),
            pltpu.VMEM(pixels.shape, bf16),
            pltpu.SemaphoreType.DMA((3,)),
        ],
        compiler_params=roomy(12),
        name="pack",
    )(place, *held_in(pltpu.HBM, master, pixels))


def fold_pair_kernel(near_ref, got_ref, own_ref, *part_refs):
    share = own_ref.shape[0]

    def one(n, carry):
        for k in range(len(part_refs) + 1):
            total = near_ref[k * share + n].astype(f32) + got_ref[k * share + n].astype(f32)
            if k == 0:
                own_ref[n] = total
            else:
                part_refs[k - 1][n] = total.astype(bf16)
        return carry

    lax.fori_loop(0, share, one, 0, unroll=4)


def fold_pair(near, got, groups):
    shape = ((near.shape[0] - 1) // groups,) + near.shape[1:]
    return pl.pallas_call(
        fold_pair_kernel,
        in_specs=[VMEM_BLOCK] * 2,
        out_specs=[VMEM_BLOCK] * groups,
        out_shape=[pltpu.VMEM(shape, f32)] + [pltpu.VMEM(shape, bf16)] * (groups - 1),
        compiler_params=roomy(4),
        name="fold_pair",
    )(*held_in(pltpu.VMEM, near, got))


def fold_tile_kernel(pieces, spot_ref, *refs):
    piece_refs, refs = refs[:pieces], refs[pieces:]
    vector_refs, refs = refs[:pieces], refs[pieces:]
    out_refs, sum_ref = refs[:-1], refs[-1]
    groups = len(out_refs)
    share = out_refs[0].shape[0]
    owned = piece_refs[0].shape[0]
    total = vector_refs[0][...]
    for ref in vector_refs[1:]:
        total = total + ref[...]
    for n in range(sum_ref.shape[0]):
        sum_ref[n] = jnp.zeros((HALF, 128), f32)
    for n in range(VEC_BLOCKS):
        sum_ref[n] = total[n * HALF : (n + 1) * HALF]

    def one(n, carry):
        for k, out_ref in enumerate(out_refs):
            number = lax.rem(spot_ref[0] + k, groups) * share + n
            block = jnp.minimum(number, owned - 1)
            total = piece_refs[0][block].astype(f32)
            for ref in piece_refs[1:]:
                total = total + ref[block].astype(f32)
            rest = sum_ref[jnp.maximum(number - owned, 0)]
            out_ref[n] = jnp.where(number < owned, total, rest).astype(out_ref.dtype)
        return carry

    lax.fori_loop(0, share, one, 0, unroll=share <= 16)


def fold_tile(spot, pieces, vectors, extra, groups):
    shape = ((pieces[0].shape[0] + extra) // groups,) + pieces[0].shape[1:]
    return pl.pallas_call(
        functools.partial(fold_tile_kernel, len(pieces)),
        in_specs=[SMEM] + [VMEM_BLOCK] * (len(pieces) + len(vectors)),
        out_specs=[VMEM_BLOCK] * groups,
        out_shape=[pltpu.VMEM(shape, f32)] + [pltpu.VMEM(shape, bf16)] * (groups - 1),
        scratch_shapes=[pltpu.VMEM((extra, HALF, 128), f32)],
        compiler_params=roomy(8),
        name="fold_tile",
    )(spot, *held_in(pltpu.VMEM, *pieces, *vectors))


def fold_batch_kernel(owned, vector_weight, spot_ref, *refs):
    part_refs, (total_ref, norm_ref) = refs[:-2], refs[-2:]
    share = total_ref.shape[0]
    square = jnp.zeros((8, 128), f32)
    for n in range(share):
        total = part_refs[0][n].astype(f32)
        for ref in part_refs[1:]:
            total = total + ref[n].astype(f32)
        total_ref[n] = total.astype(bf16)
        weight = jnp.where(spot_ref[0] * share + n < owned, 1.0, vector_weight)
        square = square + weight * fold(total * total)
    square = jnp.sum(jnp.sum(square, axis=1, keepdims=True), axis=0, keepdims=True)
    norm_ref[...] = jnp.broadcast_to(square[None], norm_ref.shape)


def fold_batch(spot, parts, owned, tile_count):
    count = tile_count * len(parts)
    return pl.pallas_call(
        functools.partial(fold_batch_kernel, owned, 1.0 / tile_count),
        in_specs=[SMEM] + [VMEM_BLOCK] * len(parts),
        out_specs=[VMEM_BLOCK] * 2,
        out_shape=[pltpu.VMEM(parts[0].shape, bf16), pltpu.VMEM((count, 1, 128), f32)],
        name="fold_batch",
    )(spot, *held_in(pltpu.VMEM, *parts))


def update_kernel(owned, groups, spot_ref, norm_ref, *refs):
    quarters, refs = refs[:groups], refs[groups:]
    stat_hbm, out_hbm, (vector_ref, clip_ref), refs = refs[:5], refs[5:10], refs[10:12], refs[12:]
    stat_refs, out_refs, (in_sem, out_sem) = refs[:5], refs[5:10], refs[10:]
    master_ref, left_stat_ref, right_stat_ref, left_root_ref, right_root_ref = stat_refs
    grad_ref, left_ref, right_ref, new_ref, copy_ref = out_refs
    share = quarters[0].shape[0]
    spans = spans_of(owned)

    def copies_of(sources, targets, sems):
        return [
            [
                pltpu.make_async_copy(
                    source.at[pl.ds(*span)], target.at[pl.ds(*span)], sems.at[5 * n + k]
                )
                for k, (source, target) in enumerate(zip(sources, targets))
            ]
            for n, span in enumerate(spans)
        ]

    copies_in = copies_of(stat_hbm, stat_refs, in_sem)
    copies_out = copies_of(out_refs, out_hbm, out_sem)
    for copies in copies_in:
        for copy in copies:
            copy.start()
    norm = jnp.sqrt(jnp.sum(norm_ref[...], axis=0))
    factor = jnp.minimum(1.0, clip_limit / norm)
    left_half = lax.broadcasted_iota(jnp.int32, (HALF, 128), 1) < BS

    def summed(number):
        source = number // share
        local = number - source * share
        turn = lax.rem(spot_ref[0] - source + groups, groups)
        value = quarters[0][local].astype(f32)
        for k in range(1, groups):
            value = jnp.where(turn == k, quarters[k][local].astype(f32), value)
        return value * factor

    def side_by_side(first, count):
        sides = []
        for n in range(first, first + count, 2):
            dense = summed(n)
            turned = pltpu.roll(dense, BS, 1)
            if n + 1 < first + count:
                second = summed(n + 1)
                top = jnp.where(left_half, dense, pltpu.roll(second, BS, 1))
                low = jnp.where(left_half, turned, second)
                side = jnp.concatenate([top, low], axis=0)
                grad_ref[n + 1] = pltpu.roll(side, BS, 1)[:, :BS]
            else:
                side = jnp.concatenate([dense, turned], axis=0)[:, :BS]
            grad_ref[n] = side[:, :BS]
            sides.append(side.astype(bf16))
        return jnp.concatenate(sides, axis=1)

    def diagonal_of(count):
        order = (count * BS, count * BS)
        return lax.broadcasted_iota(jnp.int32, order, 0) // BS == (
            lax.broadcasted_iota(jnp.int32, order, 1) // BS
        )

    clip_ref[...] = norm
    for n in range(vector_ref.shape[0]):
        vector_ref[n] = summed(owned + n)
    for (first, length), arriving, leaving in zip(spans, copies_in, copies_out):
        parts = [(n, min(4, first + length - n)) for n in range(first, first + length, 4)]
        wides = [side_by_side(*part) for part in parts]
        tall = [
            jnp.where(diagonal_of(count), jnp.concatenate([wide] * count, axis=0), 0.0)
            for (_, count), wide in zip(parts, wides)
        ]
        lefts = [product_nt(one, wide) for one, wide in zip(tall, wides)]
        rights = [product_tn(wide, wide) for wide in wides]
        for copy in arriving:
            copy.wait()
        stepped = []
        for (start, count), wide in zip(parts, wides):
            roots = left_root_ref[pl.ds(start, count)].reshape(count * BS, BS).astype(bf16)
            stepped.append(product(roots, wide))
        for (start, count), left, right in zip(parts, lefts, rights):
            here = pl.ds(start, count)
            left_ref[here] = 0.5 * left_stat_ref[here] + 0.5 * left.reshape(count, BS, BS)
            for n in range(count):
                at = n // 2 * 128
                block = right[n * BS : n * BS + BS, at : min(at + 128, count * BS)]
                if n % 2:
                    block = pltpu.roll(block, BS, 1)
                right_ref[start + n] = 0.5 * right_stat_ref[start + n] + 0.5 * block[:, :BS]
        for (start, count), value in zip(parts, stepped):
            here = pl.ds(start, count)
            value = jnp.where(diagonal_of(count), value, 0.0).astype(bf16)
            roots = right_root_ref[here].reshape(count * BS, BS).astype(bf16)
            value = product(value, roots).reshape(count, BS, BS)
            new = master_ref[here] - rate_matrix * value
            new_ref[here] = new
            copy_ref[here] = new.astype(bf16)
        for copy in leaving:
            copy.start()
    for leaving in copies_out:
        for copy in leaving:
            copy.wait()


def spans_of(owned):
    spans = []
    first = 0
    while first < owned:
        length = min(8 if first == 0 else 12, owned - first)
        spans.append((first, length))
        first += length
    return spans


def update(spot, norm, quarters, extra, *stats):
    shape = stats[0].shape
    groups = len(quarters)
    types = [f32] * 4 + [bf16]
    steps = len(spans_of(shape[0]))
    return pl.pallas_call(
        functools.partial(update_kernel, shape[0], groups),
        in_specs=[SMEM] + [VMEM_BLOCK] * (groups + 1) + [HBM] * 5,
        out_specs=[HBM] * 5 + [VMEM_BLOCK] * 2,
        out_shape=[pltpu.HBM(shape, kind) for kind in types]
        + [
            pltpu.VMEM((extra, HALF, 128), f32),
            pltpu.VMEM((1, 128), f32),
        ],
        scratch_shapes=[pltpu.VMEM(shape, f32)] * 5
        + [pltpu.VMEM(shape, kind) for kind in types]
        + [
            pltpu.SemaphoreType.DMA((5 * steps,)),
            pltpu.SemaphoreType.DMA((5 * steps,)),
        ],
        compiler_params=roomy(20),
        name="update",
    )(spot, *held_in(pltpu.VMEM, norm, *quarters), *held_in(pltpu.HBM, *stats))


def share_out(pieces, axis):
    return lax.all_to_all(pieces, axis, split_axis=0, concat_axis=0, tiled=True)


def swap(piece, distance):
    count = lax.axis_size("tile")
    return lax.ppermute(piece, "tile", [(i, i ^ distance) for i in range(count)])


def on_device(
    pixels,
    buckets,
    slot_owner_table,
    out_grad,
    master,
    left_stat,
    right_stat,
    left_root,
    right_root,
    vectors,
    moment,
):
    tile_count = lax.axis_size("tile")
    tile_place = lax.axis_index("tile")
    slot_count = pixels.shape[2]
    group_count = tile_count // STRIPS
    pairs = group_count // 2
    owned = master.shape[0]
    slots = owned * tile_count
    batch_count = lax.axis_size("batch")
    spot = lax.axis_index("batch").astype(jnp.int32).reshape(1)
    extra = extra_of(owned, batch_count)
    place = tile_place.astype(jnp.int32).reshape(1)
    paired = tile_count == 8
    numbers = jnp.arange(slots, dtype=jnp.int32)
    slot_of = jnp.sum(
        jnp.where(slot_owner_table[None, :] == numbers[:, None], numbers[None, :], 0), axis=1
    )
    if paired:
        owner = slot_of // owned
        apart = owner ^ tile_place
        apart = (apart & 1) * (tile_count // 2) + (apart >> 1)
        slot_of = slot_of + owned * (apart - owner)
    half = slots // 2
    near_place = jnp.where(slot_of < half, slot_of, half)
    far_place = jnp.where(slot_of < half, half, slot_of - half)
    vec = vectors.reshape(-1, 128)
    turned = lax.dynamic_index_in_dim(
        buckets.reshape(group_count, slot_count), tile_place, 1, keepdims=False
    ) >= 2
    flips = turned.reshape(-1, 1, 1, 1)
    goal = out_grad.reshape(2 * pairs, H3, W3, C3)
    goal = jnp.where(flips, goal.transpose(0, 2, 1, 3), goal)[:, :LINES]
    goal = goal.reshape(pairs, 2, LINES, W3, C3).transpose(0, 2, 3, 1, 4)
    goal = goal.reshape(pairs, LINES, 2 * W3, C3)
    goal = jnp.pad(goal, ((0, 0), (0, 0), (0, LINE - 2 * W3), (0, WIDE - C3)))
    goal = goal.reshape(pairs, AREA, WIDE)

    if paired:
        own, for_x, for_y, for_both = pack_pieces(
            place, master, pixels[0, 0].transpose(1, 2, 0, 3)
        )
        from_x, from_y, strips_both = swap(for_x, 2), swap(for_y, 4), swap(for_both, 6)
        goal, vec, slot_of, near_place, far_place, from_x = lax.optimization_barrier(
            (goal, vec, slot_of, near_place, far_place, from_x)
        )
        near_half = (owned + 1) // 2
        middle = STRIP_ROWS + near_half * HALF
        first_half = swap(from_x[STRIP_ROWS:middle], 4)
        second_half = swap(from_y[middle : STRIP_ROWS + owned * HALF], 2)
        mine = [own, from_x, from_y, strips_both, first_half, second_half]
        both = mine + [swap(piece, 1) for piece in mine]
        strips = both[:4] + both[6:10]
        pieces = [both[n] for n in (0, 1, 2, 4, 5, 6, 7, 8, 10, 11)]
        spans = [(STRIP_ROWS, owned)] * 3 + [(0, near_half), (0, owned - near_half)]
        spans = spans * 2
    else:
        pieces = [lax.all_gather(pack(master), "tile", axis=0, tiled=True).reshape(-1, 2 * BS)]
        spans = [(0, slots)]
        strips = share_out(pixels.reshape(tile_count, STRIP, C2), "tile")
        strips = [jnp.pad(strips, ((0, 0), (0, STRIP_ROWS - STRIP), (0, 0)))]

    weights = run_unpack(slot_of, pieces, spans)
    state = run_entry(place, buckets, strips, vec, tile_count)
    result, *back, near, far, flat = run_main(
        (near_place, far_place),
        place,
        buckets,
        state,
        goal,
        vec,
        weights,
        tile_count,
    )
    pixel_back, vector = run_exit(place, buckets, state, back, flat, vec, tile_count)
    if paired:
        own, *parts = fold_pair(near, swap(far, 1), tile_count // 2)
        pieces = [own] + [swap(part, 2 * k + 2) for k, part in enumerate(parts)]
        vector, _ = lax.optimization_barrier((vector, parts[0]))
        vector = vector + swap(vector, 1)
        vectors_in = [vector] + [swap(vector, 2 * k) for k in range(1, tile_count // 2)]
    else:
        outgoing = jnp.concatenate([near[:half], far[:half]], axis=0)
        pieces = list(share_out(outgoing.reshape(tile_count, owned, HALF, 128), "tile"))
        vectors_in = list(lax.all_gather(vector, "tile"))
    result, pieces[1] = lax.optimization_barrier((result, pieces[1]))
    result = result.reshape(pairs, LINES, LINE, WIDE)[:, :, : 2 * W3, :C3]
    result = result.reshape(pairs, LINES, W3, 2, C3).transpose(0, 3, 1, 2, 4)
    result = result.reshape(2 * pairs, LINES, W3, C3)
    result = jnp.pad(result, ((0, 0), (0, H3 - LINES), (0, 0), (0, 0)))
    result = jnp.where(flips, result.transpose(0, 2, 1, 3), result)
    result = result.reshape(out_grad.shape)
    result = with_layout_constraint(result, Layout(major_to_minor=(0, 1, 2, 4, 5, 3, 6)))
    result, vectors_in[0] = lax.optimization_barrier((result, vectors_in[0]))
    own, *parts = fold_tile(spot, pieces, vectors_in, extra, batch_count)
    pixel_back, parts[0] = lax.optimization_barrier((pixel_back, parts[0]))
    returned = share_out(pixel_back, "tile")
    parts = [
        lax.ppermute(part, "batch", [(i, (i + k + 1) % batch_count) for i in range(batch_count)])
        for k, part in enumerate(parts)
    ]
    quarter, norm = fold_batch(spot, [own] + parts, owned, tile_count)
    returned, norm = lax.optimization_barrier((returned, norm))
    norm = share_out(norm, ("batch", "tile"))
    returned = returned.astype(f32).reshape(pixels.shape)
    returned = with_layout_constraint(returned, Layout(major_to_minor=(0, 1, 3, 4, 2, 5)))
    returned, quarter = lax.optimization_barrier((returned, quarter))
    quarters = [quarter] + [
        lax.ppermute(quarter, "batch", [(i, (i + k) % batch_count) for i in range(batch_count)])
        for k in range(1, batch_count)
    ]
    block_grad, left_new, right_new, master_new, weight_copy, whole_vector, clip = update(
        spot, norm, quarters, extra, master, left_stat, right_stat, left_root, right_root
    )
    clip_norm = clip[0, 0]
    share = vectors.shape[0] // tile_count
    whole_vector = whole_vector.reshape(-1)
    vec_grad = lax.dynamic_slice_in_dim(whole_vector, tile_place * share, share, 0)
    vec_moment = moment + vec_grad * vec_grad
    own_vectors = lax.dynamic_slice_in_dim(vectors, tile_place * share, share, 0)
    vec_new = own_vectors - rate_vector * vec_grad / (jnp.sqrt(vec_moment) + eps_adagrad)
    return (
        result,
        returned,
        clip_norm,
        block_grad,
        left_new,
        right_new,
        master_new,
        weight_copy,
        vec_grad,
        vec_moment,
        vec_new,
    )


def solution(mesh):
    placed = (
        P("batch", "tile", None, None, None, None),
        P("batch"),
        P(),
        P("batch", "tile", None, None, None, None, None),
        P("tile", None, None),
        P("tile", None, None),
        P("tile", None, None),
        P("tile", None, None),
        P("tile", None, None),
        P(),
        P("tile"),
    )
    return jax.shard_map(
        on_device,
        mesh=mesh,
        in_specs=placed,
        out_specs=(
            P("batch", "tile", None, None, None, None, None),
            P("batch", "tile", None, None, None, None),
            P(),
            P("tile", None, None),
            P("tile", None, None),
            P("tile", None, None),
            P("tile", None, None),
            P("tile", None, None),
            P("tile"),
            P("tile"),
            P("tile"),
        ),
        check_vma=False,
    )
```

```python
import functools

import jax
import jax.numpy as jnp
from jax import lax
from jax.experimental import pallas as pl
from jax.experimental.layout import Layout, with_layout_constraint
from jax.experimental.pallas import tpu as pltpu
from jax.sharding import PartitionSpec as P

C2 = 128
HID2 = 512
C3 = 320
HID3 = 1280
CH = 36
CW = 36
STRIPS = 4
BS = 64
SR = CH // STRIPS
H3 = CH // 2
W3 = CW // 2
LONG = 7 * CH // 9
LINES = LONG // 2
WIDE = 384
LINE = 40
AREA = LINES * LINE
STEP = 2 * LINE
STEPS = AREA // STEP
HALF = BS // 2
STRIP = SR * CW
STRIP_ROWS = STRIP + -STRIP % 16

eps_norm = 1e-05
clip_limit = 1.0
rate_matrix = 0.3
rate_vector = 0.3
eps_adagrad = 1e-08
f32 = jnp.float32
bf16 = jnp.bfloat16

SHAPES = [(C2, HID2), (HID2, C2), (9 * C2, C3), (C3, HID3), (HID3, C3)]
USED = sum(rows // BS * (cols // BS) for rows, cols in SHAPES)
VEC_ROWS = (6 * C2 + HID2 + C2 + C3 + 6 * C3 + HID3 + C3) // 128


VEC_BLOCKS = -(-VEC_ROWS // HALF)


def extra_of(owned, groups):
    return VEC_BLOCKS + -(owned + VEC_BLOCKS) % groups


def product(left, right):
    return jnp.dot(left, right, preferred_element_type=f32)


def product_nt(left, right):
    return lax.dot_general(left, right, (((1,), (1,)), ((), ())), preferred_element_type=f32)


def product_tn(left, right):
    return lax.dot_general(left, right, (((0,), (0,)), ((), ())), preferred_element_type=f32)


def gelu_pair(values):
    bell = jnp.exp2(values * values * (-0.5 * 1.4426950408889634))
    step = pl.reciprocal(1.0 + (0.3275911 * 0.7071067811865476) * jnp.abs(values), approx=True)
    tail = step * (
        0.5 * 0.254829592
        + step
        * (
            0.5 * -0.284496736
            + step
            * (0.5 * 1.421413741 + step * (0.5 * -1.453152027 + step * (0.5 * 1.061405429)))
        )
    )
    tail = tail * bell
    share = jnp.where(values >= 0.0, 1.0 - tail, tail)
    return (values * share, share + values * (bell * 0.3989422804014327))


def fold(values):
    chans = values.shape[-1]
    return jnp.sum(values.reshape(-1, 8, chans), axis=0)


def by_image(total):
    total = total + pltpu.roll(total, 4, 0)
    total = total + pltpu.roll(total, 2, 0)
    return jnp.sum(total, axis=1, keepdims=True)


def line(pattern):
    return jnp.concatenate([pattern] * (LINE // 8), axis=0)


def spread(pattern, chans):
    return jnp.broadcast_to(pattern, (8, chans))


def affine(values, factor, shift):
    tiles = values.reshape(-1, 8, values.shape[-1])
    return (tiles * factor + shift).reshape(values.shape)


def scaled(values, factor):
    tiles = values.reshape(-1, 8, values.shape[-1])
    return (tiles * factor).reshape(values.shape)


def from_left(values):
    return pltpu.roll(values, 2, 0)


def from_right(values):
    return pltpu.roll(values, values.shape[0] - 2, 0)


def rounded(values):
    return values.astype(bf16).astype(f32)


def widen(values):
    return jnp.concatenate([values] * (WIDE // 128), axis=-1)


def norm_terms(total, square, count):
    mean = by_image(total) / count
    scaling = lax.rsqrt(by_image(square) / count - mean * mean + eps_norm)
    return (mean, scaling)


def sweep(visit, start):
    return lax.fori_loop(0, STEPS, visit, start, unroll=True)


def step_rows(k, lines=0):
    start = k * STEP + lines * LINE
    return pl.ds(start if isinstance(k, int) else pl.multiple_of(start, LINE), STEP)


def held_in(space, *arrays):
    return [pltpu.with_memory_space_constraint(array, space) for array in arrays]


VMEM_BLOCK = pl.BlockSpec(memory_space=pltpu.VMEM)
HBM = pl.BlockSpec(memory_space=pltpu.HBM)
SMEM = pl.BlockSpec(memory_space=pltpu.SMEM)


def roomy(mebibytes):
    return pltpu.CompilerParams(vmem_limit_bytes=mebibytes * 1024 * 1024)


def image_shape(bucket_of, pair, image):
    bucket = bucket_of(2 * pair + image)
    plain = jnp.where(bucket == 0, 5 * CH // 9, 7 * CH // 9)
    across = jnp.where(bucket == 0, CW, 7 * CW // 9)
    turned = (bucket >= 2).astype(jnp.int32)
    return (
        jnp.where(turned > 0, 5 * CW // 9, plain),
        jnp.where(turned > 0, CH, across),
        turned,
    )


def bucket_reader(place_ref, bucket_ref, strip_count):
    return lambda group: bucket_ref[group * strip_count + place_ref[0]]


class Geometry:
    def __init__(self, bucket_of, pair):
        parity = lax.broadcasted_iota(jnp.int32, (8, 128), 0) % 2
        even, odd = (image_shape(bucket_of, pair, image) for image in range(2))
        high, broad, turned = (jnp.where(parity == 0, a, b) for a, b in zip(even, odd))
        self.high = high
        self.count_two = (high * broad * C2).astype(f32)[:, :1]
        self.high3 = (high + 1) // 2
        broad3 = (broad + 1) // 2
        self.count_three = (self.high3 * broad3 * C3).astype(f32)[:, :1]
        place = lax.broadcasted_iota(jnp.int32, (LINE, 128), 0) // 2
        inside = lax.broadcasted_iota(jnp.int32, (LINE, 128), 0) < 2 * W3
        self.reach = []
        self.col_share = []
        for pc in range(2):
            column = 2 * place + pc
            self.reach.append(jnp.where(inside & (column < line(broad)), line(high), 0))
            edge = (column == 0) | (column == line(broad) - 1)
            self.col_share.append(jnp.where(edge, 0.5, 1.0 / 3.0))
        self.reach3 = jnp.where(inside & (place < line(broad3)), line(self.high3), 0)
        edge3 = (place == 0) | (place == line(broad3) - 1)
        self.col_share3 = jnp.where(edge3, 0.5, 1.0 / 3.0)
        self.flipped = jnp.concatenate([turned] * (STEP // 8), axis=0) > 0

    def share(self, plane, k):
        pr, pc = plane // 2, plane % 2
        return self.lines(4 * k + pr, 2, self.reach[pc], self.col_share[pc], self.high)

    def share3(self, k):
        return self.lines(2 * k, 1, self.reach3, self.col_share3, self.high3)

    def lines(self, row, stride, reach, col_share, height):
        parts = []
        for n in range(2):
            here = row + stride * n
            row_share = jnp.where((here == 0) | (here == height - 1), 0.5, 1.0 / 3.0)
            parts.append(jnp.where(here < reach, line(row_share) * col_share, 0.0))
        return jnp.concatenate(parts, axis=0)


def strip_place(pair, spot, strip_count):
    return lax.rem(pair * 8 + strip_count - 2 + spot, strip_count)


def each_image(bucket_of, pair, visit):
    for image in range(2):
        way = image_shape(bucket_of, pair, image)[2]

        @pl.when(way == 0)
        def _():
            def one(r, carry):
                for plane in range(4):
                    row = 2 * r + plane // 2
                    strip = row // SR
                    there = pl.ds((row - strip * SR) * CW + plane % 2, W3, stride=2)
                    here = pl.ds(r * LINE + image, W3, stride=2)
                    visit(plane, here, image * STRIPS + strip, there)
                return carry

            lax.fori_loop(0, LINES, one, 0)

        @pl.when(way == 1)
        def _():
            def one(r, carry):
                for plane in range(4):
                    for strip in range(STRIPS):
                        first = (plane % 2 + strip * SR) % 2
                        count = (SR - first + 1) // 2
                        done = (strip * SR + first) // 2
                        column = 2 * r + plane // 2
                        there = pl.ds(first * CW + column, count, stride=2 * CW)
                        here = pl.ds(r * LINE + image + 2 * done, count, stride=2)
                        visit(plane, here, image * STRIPS + strip, there)
                return carry

            lax.fori_loop(0, LINES, one, 0)


def row_windows(col_ref, pc, k):
    both = col_ref[pc, step_rows(k, 1)] + col_ref[2 + pc, step_rows(k, 1)]
    return (both + col_ref[2 + pc, step_rows(k)], both + col_ref[pc, step_rows(k, 2)])


def put_col_windows(col_ref, pr, k, even, odd):
    both = even + odd
    col_ref[pr * 2, step_rows(k, 1)] = both + from_left(odd)
    col_ref[pr * 2 + 1, step_rows(k, 1)] = both + from_right(even)


def clear_edges(col_ref):
    zero_line = jnp.zeros((LINE, C2), f32)
    for plane in range(4):
        col_ref[plane, 0:LINE] = zero_line
        col_ref[plane, AREA + LINE : AREA + 2 * LINE] = zero_line


def entry_kernel(pairs, strip_count, piece_count, place_ref, bucket_ref, vec_ref, *refs):
    piece_refs, refs = refs[:piece_count], refs[piece_count:]
    x_out, inv_out, pool_out, mix_out, stat_out, image_ref, col_ref = refs
    pair = pl.program_id(0) if pairs > 1 else 0
    x_ref, inv_ref, pool_ref, mix_ref = (ref.at[0] for ref in (x_out, inv_out, pool_out, mix_out))
    bucket_of = bucket_reader(place_ref, bucket_ref, strip_count)
    shape = Geometry(bucket_of, pair)
    gain1, bias1, scale1 = (vec_ref[n : n + 1] for n in range(3))
    clear_edges(col_ref)
    if piece_count > 1:
        half = piece_count // 2
        for n, ref in enumerate(piece_refs):
            source = place_ref[0] ^ (n // half + 2 * (n % half))
            spot = lax.rem(source + 2, 2 * STRIPS)
            first = 0 if n < half else ref.shape[0] - STRIP_ROWS
            image_ref[spot] = ref[first : first + STRIP_ROWS].astype(f32)
    else:
        for spot in range(2 * STRIPS):
            source = strip_place(pair, spot, strip_count)
            image_ref[spot] = piece_refs[0][source].astype(f32)

    def take_in(plane, here, spot, there):
        x_ref[plane, here] = image_ref[spot, there]

    each_image(bucket_of, pair, take_in)

    def arrange(k, carry):
        total, square = carry
        rows = step_rows(k)
        for plane in range(4):
            share = shape.share(plane, k)
            inv_ref[plane, rows] = share
            values = jnp.where(share > 0.0, x_ref[plane, rows], 0.0)
            x_ref[plane, rows] = values
            total = total + fold(values)
            square = square + fold(values * values)
        return (total, square)

    nothing = jnp.zeros((8, C2), f32)
    total, square = sweep(arrange, (nothing, nothing))
    mean1, scaling1 = norm_terms(total, square, shape.count_two)
    factor1 = scaling1 * gain1
    shift1 = bias1 - mean1 * scaling1 * gain1

    def window_cols(k, carry):
        rows = step_rows(k)
        for pr in range(2):
            masked = []
            for pc in range(2):
                plane = pr * 2 + pc
                normal = rounded(affine(x_ref[plane, rows], factor1, shift1))
                masked.append(jnp.where(inv_ref[plane, rows] > 0.0, normal, 0.0))
            put_col_windows(col_ref, pr, k, *masked)
        return carry

    sweep(window_cols, 0)

    def mix(k, carry):
        total, square = carry
        rows = step_rows(k)
        for pc in range(2):
            windows = row_windows(col_ref, pc, k)
            for pr in range(2):
                plane = pr * 2 + pc
                values = x_ref[plane, rows]
                share = inv_ref[plane, rows]
                pooled = windows[pr] * share - rounded(affine(values, factor1, shift1))
                pooled = jnp.where(share > 0.0, pooled, 0.0)
                mixed = values + scale1 * pooled
                pool_ref[plane, rows] = pooled
                mix_ref[plane, rows] = mixed
                total = total + fold(mixed)
                square = square + fold(mixed * mixed)
        return (total, square)

    total, square = sweep(mix, (nothing, nothing))
    mean2, scaling2 = norm_terms(total, square, shape.count_two)
    for n, value in enumerate((mean1, scaling1, mean2, scaling2)):
        stat_out[0, n] = spread(value, 128)


def pair_specs(pairs, shapes, mode=None):
    if pairs == 1:
        return [VMEM_BLOCK] * len(shapes)
    return [
        pl.BlockSpec(
            (1,) + shape, lambda t, rank=len(shape): (t,) + (0,) * rank, pipeline_mode=mode
        )
        for shape in shapes
    ]


def whole_specs(pairs, shapes):
    if pairs == 1:
        return [VMEM_BLOCK] * len(shapes)
    return [
        pl.BlockSpec(
            shape,
            lambda t, rank=len(shape): (0,) * rank,
            pipeline_mode=pl.Buffered(1),
        )
        for shape in shapes
    ]


def pair_arrays(pairs, shapes, kinds):
    make = pltpu.VMEM if pairs == 1 else jax.ShapeDtypeStruct
    return [make((pairs,) + shape, kind) for shape, kind in zip(shapes, kinds)]


STATE = [(4, AREA, C2)] * 4 + [(4, 8, 128)]
BACK = [(4, AREA, C2)] * 2 + [(2, 8, 128)]


def run_entry(place, buckets, pieces, vec, strip_count):
    pairs = strip_count // 8
    if pairs == 1:
        pieces = held_in(pltpu.VMEM, *pieces)
    return pl.pallas_call(
        functools.partial(entry_kernel, pairs, strip_count, len(pieces)),
        grid=() if pairs == 1 else (pairs,),
        in_specs=[SMEM] * 2 + whole_specs(pairs, [array.shape for array in (vec, *pieces)]),
        out_specs=pair_specs(pairs, STATE),
        out_shape=pair_arrays(pairs, STATE, [f32] * 5),
        scratch_shapes=[
            pltpu.VMEM((2 * STRIPS, STRIP_ROWS, C2), f32),
            pltpu.VMEM((4, AREA + 2 * LINE, C2), f32),
        ],
        compiler_params=roomy(6 if pairs == 1 else 40),
        name="entry",
    )(place, buckets, vec, *pieces)


WEIGHTS = [(C2, HID2), (HID2, C2), (9 * C2, WIDE), (WIDE, HID3), (HID3, WIDE)]


def unpack_kernel(spans, slot_ref, *refs):
    piece_refs, refs = refs[: len(spans)], refs[len(spans) :]
    weights, gathered_ref = refs[:-1], refs[-1]
    done = 0
    for ref, (first, count) in zip(piece_refs, spans):
        blocks = ref[first : first + count * HALF].reshape(count, HALF, 128)
        gathered_ref[done : done + count] = blocks
        done += count
    left_half = lax.broadcasted_iota(jnp.int32, (HALF, 128), 1) < BS
    offset = 0
    for (rows, cols), ref in zip(SHAPES, weights):
        wide = cols // BS
        for rb in range(rows // BS):
            for cb in range(0, wide, 2):
                number = offset + rb * wide + cb
                first = gathered_ref[slot_ref[number]]
                turned = pltpu.roll(first, BS, 1)
                if cb + 1 < wide:
                    second = gathered_ref[slot_ref[number + 1]]
                    top = jnp.where(left_half, first, pltpu.roll(second, BS, 1))
                    low = jnp.where(left_half, turned, second)
                else:
                    top = jnp.where(left_half, first, 0.0)
                    low = jnp.where(left_half, turned, 0.0)
                place = slice(cb * BS, cb * BS + 128)
                ref[rb * BS : rb * BS + HALF, place] = top
                ref[rb * BS + HALF : rb * BS + BS, place] = low
        offset += rows // BS * wide
    weights[3][C3:, :] = jnp.zeros((WIDE - C3, HID3), bf16)


def run_unpack(slot_of, pieces, spans):
    slots = slot_of.shape[0]
    return pl.pallas_call(
        functools.partial(unpack_kernel, spans),
        in_specs=[SMEM] + [VMEM_BLOCK] * len(pieces),
        out_specs=[VMEM_BLOCK] * 5,
        out_shape=[pltpu.VMEM(shape, bf16) for shape in WEIGHTS],
        scratch_shapes=[pltpu.VMEM((slots, HALF, 128), bf16)],
        compiler_params=roomy(6),
        name="unpack",
    )(slot_of, *held_in(pltpu.VMEM, *pieces))


def main_kernel(
    pairs,
    strip_count,
    slots,
    near_place,
    far_place,
    place_ref,
    bucket_ref,
    inv_in,
    mix_in,
    stat_in,
    goal_ref,
    vec_ref,
    w1_ref,
    w2_ref,
    we_ref,
    w3_ref,
    w4_ref,
    result_ref,
    zed_out,
    dx_out,
    mean_out,
    near_ref,
    far_ref,
    flat_ref,
    zed_ref,
    hid_ref,
    u_ref,
    g_ref,
    h_ref,
    dy_ref,
    patch_ref,
    dpatch_ref,
    inv3_ref,
    e_ref,
    col3_ref,
    pool3_ref,
    mix3_ref,
    dx3_ref,
    hid3_ref,
    dhid3_ref,
    u3_ref,
    g3_ref,
    h3_ref,
    dy3_ref,
    dpre_ref,
    gw1_ref,
    gw2_ref,
    gwe_ref,
    gw3_ref,
    gw4_ref,
    acc_two,
    acc_hid_two,
    acc_three,
    acc_hid_three,
):
    pair = pl.program_id(0) if pairs > 1 else 0
    grads = [gw1_ref, gw2_ref, gwe_ref, gw3_ref, gw4_ref]
    inv_ref, mix_ref, stat_ref = (ref.at[0] for ref in (inv_in, mix_in, stat_in))
    back_ref, dx_ref = zed_out.at[0], dx_out.at[0]
    left_half = lax.broadcasted_iota(jnp.int32, (HALF, 128), 1) < BS

    def at_pair(number, act):
        if pairs == 1:
            act()
        else:
            pl.when(pair == number)(act)

    def begin():
        acc_two[...] = jnp.zeros(acc_two.shape, f32)
        acc_hid_two[...] = jnp.zeros(acc_hid_two.shape, f32)
        acc_three[...] = jnp.zeros(acc_three.shape, f32)
        acc_hid_three[...] = jnp.zeros(acc_hid_three.shape, f32)

    at_pair(0, begin)
    shape = Geometry(bucket_reader(place_ref, bucket_ref, strip_count), pair)
    count_two, count_three, flipped = shape.count_two, shape.count_three, shape.flipped
    nothing = jnp.zeros((8, C2), f32)
    nothing3 = jnp.zeros((8, WIDE), f32)

    def vector_row(at, length):
        first, shift = at // 128, at % 128
        count = -(-(shift + length) // 128)
        row = jnp.concatenate([vec_ref[first + n : first + n + 1] for n in range(count)], axis=1)
        if shift:
            row = pltpu.roll(jnp.broadcast_to(row, (8, count * 128)), count * 128 - shift, 1)[:1]
        return row

    def wide_row(at):
        lane = lax.broadcasted_iota(jnp.int32, (1, WIDE), 1)
        return jnp.where(lane < C3, vector_row(at, C3)[:, :WIDE], 0.0)

    gain2, bias2, scale2 = (vec_ref[n : n + 1] for n in range(3, 6))
    hid_bias = vector_row(6 * C2, HID2)
    out_bias = vector_row(6 * C2 + HID2, C2)
    two = 7 * C2 + HID2
    embed_bias, gain3, bias3, scale3 = (wide_row(two + n * C3) for n in range(4))
    gain4, bias4, scale4 = (wide_row(two + n * C3) for n in range(4, 7))
    hid_bias3 = vector_row(two + 7 * C3, HID3)[:, :HID3]
    out_bias3 = wide_row(two + 7 * C3 + HID3)
    mean2, scaling2 = stat_ref[2], stat_ref[3]
    factor2 = scaling2 * gain2
    shift2 = bias2 - mean2 * scaling2 * gain2
    for plane in range(4):
        zed_ref[plane, 0:LINE] = jnp.zeros((LINE, C2), f32)
    col3_ref[0:LINE] = jnp.zeros((LINE, WIDE), f32)
    col3_ref[AREA + LINE : AREA + 2 * LINE] = jnp.zeros((LINE, WIDE), f32)

    def put_block(number, block):
        near_ref[near_place[number]] = block
        far_ref[far_place[number]] = block

    def pack_blocks(matrices):
        offsets = [0]
        for rows, cols in SHAPES:
            offsets.append(offsets[-1] + rows // BS * (cols // BS))
        for which in matrices:
            (rows, cols), ref = SHAPES[which], grads[which]
            wide = cols // BS
            for rb in range(rows // BS):
                for cb in range(0, wide, 2):
                    number = offsets[which] + rb * wide + cb
                    at = slice(cb * BS, cb * BS + 128)
                    top = ref[rb * BS : rb * BS + HALF, at].astype(bf16)
                    low = ref[rb * BS + HALF : rb * BS + BS, at].astype(bf16)
                    put_block(number, jnp.where(left_half, top, pltpu.roll(low, BS, 1)))
                    if cb + 1 < wide:
                        put_block(number + 1, jnp.where(left_half, pltpu.roll(top, BS, 1), low))

    def plane_rows(plane):
        return slice(plane * AREA, plane * AREA + AREA)

    def begin_plane(plane):
        low = affine(mix_ref[plane], factor2, shift2).astype(bf16)
        h_ref[plane_rows(plane)] = low
        hid_ref[plane % 2] = product(low, w1_ref[...])

    begin_plane(0)
    for plane in range(4):
        if plane < 3:
            begin_plane(plane + 1)
        for k in range(STEPS):
            rows = step_rows(k)
            flat = slice(plane * AREA + k * STEP, plane * AREA + k * STEP + STEP)
            for at in range(0, HID2, 128):
                lanes = slice(at, at + 128)
                active, slope = gelu_pair(hid_ref[plane % 2, rows, lanes] + hid_bias[:, lanes])
                u_ref[flat, lanes] = active.astype(bf16)
                g_ref[flat, lanes] = slope.astype(bf16)
        out = product(u_ref[plane_rows(plane)], w2_ref[...]) + out_bias
        zed = jnp.where(inv_ref[plane] > 0.0, mix_ref[plane] + scale2 * out, 0.0)
        zed_ref[plane, LINE : LINE + AREA] = rounded(zed)

    def patches(k, carry):
        rows = step_rows(k)
        taps = []
        for ky in range(3):
            pr = (0 if ky == 1 else 1) * 2
            source = step_rows(k, 0 if ky == 0 else 1)
            even = zed_ref[pr, source]
            odd = zed_ref[pr + 1, source]
            taps.append((from_left(odd), even, odd))
        for ky in range(3):
            for kx in range(3):
                at = (3 * ky + kx) * C2
                tap = taps[ky][kx]
                if ky != kx:
                    tap = jnp.where(flipped, taps[kx][ky], tap)
                patch_ref[rows, at : at + C2] = tap.astype(bf16)
        return carry

    sweep(patches, 0)
    e_ref[...] = product(patch_ref[...], we_ref[...])

    def embed(k, carry):
        total, square = carry
        rows = step_rows(k)
        share = shape.share3(k)
        inv3_ref[rows] = share
        out = jnp.where(widen(share) > 0.0, e_ref[rows] + embed_bias, 0.0)
        e_ref[rows] = out
        return (total + fold(out), square + fold(out * out))

    total, square = sweep(embed, (nothing3, nothing3))
    mean3, scaling3 = norm_terms(total, square, count_three)
    factor3 = scaling3 * gain3
    shift3 = bias3 - mean3 * scaling3 * gain3

    def window_cols3(k, carry):
        rows = step_rows(k)
        normal = rounded(affine(e_ref[rows], factor3, shift3))
        masked = jnp.where(widen(inv3_ref[rows]) > 0.0, normal, 0.0)
        col3_ref[step_rows(k, 1)] = masked + from_left(masked) + from_right(masked)
        return carry

    sweep(window_cols3, 0)

    def row_windows3(k):
        return col3_ref[step_rows(k)] + col3_ref[step_rows(k, 1)] + col3_ref[step_rows(k, 2)]

    def mix3(k, carry):
        total, square = carry
        rows = step_rows(k)
        values = e_ref[rows]
        share = widen(inv3_ref[rows])
        pooled = row_windows3(k) * share - rounded(affine(values, factor3, shift3))
        pooled = jnp.where(share > 0.0, pooled, 0.0)
        mixed = values + scale3 * pooled
        pool3_ref[rows] = pooled
        mix3_ref[rows] = mixed
        return (total + fold(mixed), square + fold(mixed * mixed))

    total, square = sweep(mix3, (nothing3, nothing3))
    mean4, scaling4 = norm_terms(total, square, count_three)
    factor4 = scaling4 * gain4
    shift4 = bias4 - mean4 * scaling4 * gain4
    normal4 = (spread(scaling4, WIDE), spread(-mean4 * scaling4, WIDE))

    def prepare3(k, d_bias):
        rows = step_rows(k)
        h3_ref[rows] = affine(mix3_ref[rows], factor4, shift4).astype(bf16)
        goal = goal_ref[0, rows].astype(f32)
        goal = jnp.where(widen(inv3_ref[rows]) > 0.0, goal, 0.0)
        low_goal = (scale4 * goal).astype(bf16)
        dy3_ref[rows] = low_goal
        return d_bias + fold(low_goal.astype(f32))

    acc_three[7] += sweep(prepare3, nothing3)

    def keep(ref, value, place=slice(None)):
        if pairs == 1:
            ref[place] = value.astype(ref.dtype)
        else:

            @pl.when(pair == 0)
            def _():
                ref[place] = value

            @pl.when(pair > 0)
            def _():
                ref[place] += value

    def begin_chunk(at):
        lanes = slice(at, at + 256)
        hid3_ref[:, lanes] = product(h3_ref[...], w3_ref[:, lanes])
        dhid3_ref[:, lanes] = product_nt(dy3_ref[...], w4_ref[lanes])

    begin_chunk(0)
    for at in range(0, HID3, 256):
        if at + 256 < HID3:
            begin_chunk(at + 256)
        for lane in (at, at + 128):
            lanes = slice(lane, lane + 128)
            total = nothing
            for k in range(STEPS):
                rows = step_rows(k)
                active, slope = gelu_pair(hid3_ref[rows, lanes] + hid_bias3[:, lanes])
                u3_ref[rows, lanes] = active.astype(bf16)
                low = (slope * dhid3_ref[rows, lanes]).astype(bf16)
                g3_ref[rows, lanes] = low
                total = total + fold(low.astype(f32))
            acc_hid_three[:, lanes] += total
        lanes = slice(at, at + 256)
        out = product(u3_ref[:, lanes], w4_ref[lanes])
        d_low = product_nt(g3_ref[:, lanes], w3_ref[:, lanes])
        result_ref[0] = out if at == 0 else result_ref[0] + out
        dx3_ref[...] = d_low if at == 0 else dx3_ref[...] + d_low
        keep(gw3_ref, product_tn(h3_ref[...], g3_ref[:, lanes]), (slice(None), lanes))
        keep(gw4_ref, product_tn(u3_ref[:, lanes], dy3_ref[...]), lanes)

    def finish3(k, carry):
        d_scale, d_shift, d_gain = carry
        rows = step_rows(k)
        valid = widen(inv3_ref[rows]) > 0.0
        mixed = mix3_ref[rows]
        out = jnp.where(valid, result_ref[0, rows] + out_bias3, 0.0)
        result_ref[0, rows] = mixed + scale4 * out
        d_scale = d_scale + fold(out * goal_ref[0, rows].astype(f32))
        d_low = dx3_ref[rows]
        normal = affine(mixed, *normal4)
        return (d_scale, d_shift + fold(d_low), d_gain + fold(d_low * normal))

    d_scale, d_shift, d_gain = sweep(finish3, (nothing3, nothing3, nothing3))
    acc_three[6] += d_scale
    acc_three[5] += d_shift
    acc_three[4] += d_gain
    mean_shift = by_image(d_shift * gain4) / count_three
    mean_gain = by_image(d_gain * gain4) / count_three
    back_gain4 = scaling4 * gain4
    back_mean4 = spread(-scaling4 * mean_shift, WIDE)
    back_normal4 = spread(scaling4 * mean_gain, WIDE)

    def unmix3(k, d_scale):
        rows = step_rows(k)
        share = widen(inv3_ref[rows])
        valid = share > 0.0
        normal = affine(mix3_ref[rows], *normal4)
        back = affine(dx3_ref[rows], back_gain4, back_mean4) - scaled(normal, back_normal4)
        d_mixed = jnp.where(valid, back + goal_ref[0, rows].astype(f32), 0.0)
        dx3_ref[rows] = d_mixed
        d_scale = d_scale + fold(pool3_ref[rows] * d_mixed)
        weighted = scale3 * d_mixed * share
        col3_ref[step_rows(k, 1)] = weighted + from_left(weighted) + from_right(weighted)
        return d_scale

    acc_three[3] += sweep(unmix3, nothing3)
    normal3 = (spread(scaling3, WIDE), spread(-mean3 * scaling3, WIDE))

    def unpool3(k, carry):
        d_shift, d_gain = carry
        rows = step_rows(k)
        valid = widen(inv3_ref[rows]) > 0.0
        d_normal = jnp.where(valid, row_windows3(k) - scale3 * dx3_ref[rows], 0.0)
        pool3_ref[rows] = d_normal
        normal = affine(e_ref[rows], *normal3)
        return (d_shift + fold(d_normal), d_gain + fold(d_normal * normal))

    d_shift, d_gain = sweep(unpool3, (nothing3, nothing3))
    acc_three[2] += d_shift
    acc_three[1] += d_gain
    mean_shift = by_image(d_shift * gain3) / count_three
    mean_gain = by_image(d_gain * gain3) / count_three
    back_gain3 = scaling3 * gain3
    back_mean3 = spread(-scaling3 * mean_shift, WIDE)
    back_normal3 = spread(scaling3 * mean_gain, WIDE)

    def unnorm3(k, d_bias):
        rows = step_rows(k)
        valid = widen(inv3_ref[rows]) > 0.0
        normal = affine(e_ref[rows], *normal3)
        back = affine(pool3_ref[rows], back_gain3, back_mean3) - scaled(normal, back_normal3)
        low = jnp.where(valid, dx3_ref[rows] + back, 0.0).astype(bf16)
        dpre_ref[rows] = low
        return d_bias + fold(low.astype(f32))

    acc_three[0] += sweep(unnorm3, nothing3)
    keep(gwe_ref, product_tn(patch_ref[...], dpre_ref[...]))
    dpatch_ref[0:AREA] = product_nt(dpre_ref[...], we_ref[...])
    dpatch_ref[AREA : AREA + LINE] = jnp.zeros((LINE, 9 * C2), f32)

    def gather_back(k, carry):
        rows = step_rows(k)

        def tap(ky, kx, source):
            at = (3 * ky + kx) * C2
            value = dpatch_ref[source, at : at + C2]
            if ky != kx:
                at = (3 * kx + ky) * C2
                value = jnp.where(flipped, dpatch_ref[source, at : at + C2], value)
            return value

        sources = []
        for ky in range(3):
            source = step_rows(k, 1 if ky == 0 else 0)
            sources.append(
                (tap(ky, 1, source), tap(ky, 2, source) + from_right(tap(ky, 0, source)))
            )
        for pc in range(2):
            for pr, value in ((0, sources[1][pc]), (1, sources[2][pc] + sources[0][pc])):
                plane = pr * 2 + pc
                valid = inv_ref[plane, rows] > 0.0
                back_ref[plane, rows] = jnp.where(valid, rounded(value), 0.0)
        return carry

    sweep(gather_back, 0)

    if pairs == 1:
        pack_blocks(range(2, 5))

    normal2 = (spread(scaling2, C2), spread(-mean2 * scaling2, C2))

    def begin_back(plane):
        low_goal = (scale2 * back_ref[plane]).astype(bf16)
        dy_ref[plane_rows(plane)] = low_goal
        hid_ref[plane % 2] = product_nt(low_goal, w2_ref[...])
        return fold(low_goal.astype(f32))

    d_out_bias = begin_back(0)
    d_shift, d_gain = nothing, nothing
    sums = [nothing] * (HID2 // 128)
    new_gw1, new_gw2 = None, None
    for plane in range(4):
        if plane < 3:
            d_out_bias = d_out_bias + begin_back(plane + 1)
        for k in range(STEPS):
            rows = step_rows(k)
            part = slice(plane * AREA + k * STEP, plane * AREA + k * STEP + STEP)
            for n, at in enumerate(range(0, HID2, 128)):
                lanes = slice(at, at + 128)
                low = g_ref[part, lanes].astype(f32) * hid_ref[plane % 2, rows, lanes]
                low = low.astype(bf16)
                g_ref[part, lanes] = low
                sums[n] = sums[n] + fold(low.astype(f32))
        flat = plane_rows(plane)
        d_low = product_nt(g_ref[flat], w1_ref[...])
        dx_ref[plane] = d_low
        d_shift = d_shift + fold(d_low)
        d_gain = d_gain + fold(d_low * affine(mix_ref[plane], *normal2))
        part_gw1 = product_tn(h_ref[flat], g_ref[flat])
        part_gw2 = product_tn(dy_ref[flat], u_ref[flat])
        new_gw1 = part_gw1 if plane == 0 else new_gw1 + part_gw1
        new_gw2 = part_gw2 if plane == 0 else new_gw2 + part_gw2
    new_gw2 = new_gw2.T
    for n, value in enumerate(sums):
        acc_hid_two[:, n * 128 : n * 128 + 128] += value
    acc_two[6] += d_out_bias
    acc_two[4] += d_shift
    acc_two[3] += d_gain
    mean_out[0, 0] = spread(by_image(d_shift * gain2) / count_two, 128)
    mean_out[0, 1] = spread(by_image(d_gain * gain2) / count_two, 128)
    keep(gw1_ref, new_gw1)
    keep(gw2_ref, new_gw2)
    d_scale = fold(w2_ref[...].astype(f32) * new_gw2) + out_bias * d_out_bias
    acc_two[5] += d_scale / scale2

    def finish():
        if pairs > 1:
            pack_blocks(range(5))
        else:
            pack_blocks(range(2))

        def filler(number, carry):
            put_block(number, jnp.zeros((HALF, 128), bf16))
            return carry

        lax.fori_loop(USED, slots, filler, 0)

        flat_ref[...] = jnp.zeros(flat_ref.shape, f32)

        def put(at, total, length):
            if at % 128:
                room = jnp.zeros((8, 128), f32)
                if total.shape[1] < length + BS:
                    total = jnp.concatenate([total, room], axis=1)
                total = pltpu.roll(total, BS, 1)
            whole = jnp.sum(total, axis=0, keepdims=True)
            done = -(at % 128)
            row = at // 128
            lane = 0
            while done < length:
                first = max(0, -done)
                last = min(128, length - done)
                flat_ref[row : row + 1, first:last] = whole[:, lane + first : lane + last]
                done += 128
                lane += 128
                row += 1

        at = 3 * C2
        for n in range(3, 6):
            put(at, acc_two[n], C2)
            at += C2
        put(at, acc_hid_two[...], HID2)
        at += HID2
        put(at, acc_two[6], C2)
        at += C2
        for n in range(7):
            put(at, acc_three[n], C3)
            at += C3
        put(at, acc_hid_three[...], HID3)
        at += HID3
        put(at, acc_three[7], C3)

    at_pair(pairs - 1, finish)


def run_main(places, place, buckets, state, goal, vec, weights, strip_count):
    pairs = goal.shape[0]
    slots = places[0].shape[0]
    half = slots // 2 + 1
    if pairs == 1:
        state = held_in(pltpu.VMEM, *state)
    weights = held_in(pltpu.VMEM, *weights)
    _, inv, _, mix, stat = state
    state_shapes = [STATE[1], STATE[3], STATE[4]]
    grad_kind = bf16 if pairs == 1 else f32
    wide_f32 = pltpu.VMEM((AREA, WIDE), f32)
    wide_bf16 = pltpu.VMEM((AREA, WIDE), bf16)
    scratch = [
        pltpu.VMEM((4, AREA + LINE, C2), f32),
        pltpu.VMEM((2, AREA, HID2), f32),
        pltpu.VMEM((4 * AREA, HID2), bf16),
        pltpu.VMEM((4 * AREA, HID2), bf16),
        pltpu.VMEM((4 * AREA, C2), bf16),
        pltpu.VMEM((4 * AREA, C2), bf16),
        pltpu.VMEM((AREA, 9 * C2), bf16),
        pltpu.VMEM((AREA + LINE, 9 * C2), f32),
        pltpu.VMEM((AREA, 128), f32),
        wide_f32,
        pltpu.VMEM((AREA + 2 * LINE, WIDE), f32),
        wide_f32,
        wide_f32,
        wide_f32,
        pltpu.VMEM((AREA, HID3), f32),
        pltpu.VMEM((AREA, HID3), f32),
        pltpu.VMEM((AREA, HID3), bf16),
        pltpu.VMEM((AREA, HID3), bf16),
        wide_bf16,
        wide_bf16,
        wide_bf16,
        pltpu.VMEM((C2, HID2), grad_kind),
        pltpu.VMEM((HID2, C2), grad_kind),
        pltpu.VMEM((9 * C2, WIDE), grad_kind),
        pltpu.VMEM((WIDE, HID3), grad_kind),
        pltpu.VMEM((HID3, WIDE), grad_kind),
        pltpu.VMEM((7, 8, C2), f32),
        pltpu.VMEM((8, HID2), f32),
        pltpu.VMEM((8, 8, WIDE), f32),
        pltpu.VMEM((8, HID3), f32),
    ]
    out_shapes = [(half, HALF, 128), (half, HALF, 128), (VEC_BLOCKS * HALF, 128)]
    make = pltpu.VMEM if pairs == 1 else jax.ShapeDtypeStruct
    return pl.pallas_call(
        functools.partial(main_kernel, pairs, strip_count, slots),
        grid=() if pairs == 1 else (pairs,),
        in_specs=[SMEM] * 4
        + pair_specs(pairs, state_shapes + [goal.shape[1:]], pl.Buffered(1))
        + whole_specs(pairs, [vec.shape])
        + [VMEM_BLOCK] * 5,
        out_specs=pair_specs(pairs, [(AREA, WIDE)] + BACK) + whole_specs(pairs, out_shapes),
        out_shape=pair_arrays(pairs, [(AREA, WIDE)] + BACK, [f32] * 4)
        + [make(shape, kind) for shape, kind in zip(out_shapes, (bf16, bf16, f32))],
        scratch_shapes=scratch,
        compiler_params=pltpu.CompilerParams(
            vmem_limit_bytes=(40 if pairs == 1 else 56) * 1024 * 1024,
            fuse_transposed_lhs_in_matmul=True,
        ),
        name="blocks",
    )(*places, place, buckets, inv, mix, stat, goal, vec, *weights)


def exit_kernel(
    pairs,
    strip_count,
    place_ref,
    bucket_ref,
    x_in,
    inv_in,
    pool_in,
    mix_in,
    stat_in,
    zed_in,
    dx_in,
    mean_in,
    flat_ref,
    vec_ref,
    payload_hbm,
    vector_ref,
    payload_ref,
    image_ref,
    col_ref,
    dx_ref,
    back_ref,
    acc_ref,
    sem,
):
    pair = pl.program_id(0) if pairs > 1 else 0
    x_ref, inv_ref, pool_ref, mix_ref, stat_ref, zed_ref, low_ref, mean_ref = (
        ref.at[0] for ref in (x_in, inv_in, pool_in, mix_in, stat_in, zed_in, dx_in, mean_in)
    )
    bucket_of = bucket_reader(place_ref, bucket_ref, strip_count)
    shape = Geometry(bucket_of, pair)
    count_two = shape.count_two
    gain1, bias1, scale1, gain2 = (vec_ref[n : n + 1] for n in range(4))
    mean1, scaling1, mean2, scaling2 = (stat_ref[n] for n in range(4))
    normal2 = (scaling2, -mean2 * scaling2)
    clear_edges(col_ref)
    nothing = jnp.zeros((8, C2), f32)
    back_gain2 = scaling2 * gain2
    back_mean2 = -scaling2 * mean_ref[0]
    back_normal2 = scaling2 * mean_ref[1]

    if pairs > 1:

        @pl.when(pair == 0)
        def _():
            acc_ref[...] = jnp.zeros(acc_ref.shape, f32)

    def add_up(n, total):
        acc_ref[n] = total if pairs == 1 else acc_ref[n] + total

    def unmix(k, d_scale):
        rows = step_rows(k)
        for pr in range(2):
            weighted = []
            for pc in range(2):
                plane = pr * 2 + pc
                share = inv_ref[plane, rows]
                normal = affine(mix_ref[plane, rows], *normal2)
                back = affine(low_ref[plane, rows], back_gain2, back_mean2)
                back = back - scaled(normal, back_normal2)
                d_mixed = jnp.where(share > 0.0, zed_ref[plane, rows] + back, 0.0)
                dx_ref[plane, rows] = d_mixed
                d_scale = d_scale + fold(pool_ref[plane, rows] * d_mixed)
                weighted.append(scale1 * d_mixed * share)
            put_col_windows(col_ref, pr, k, *weighted)
        return d_scale

    add_up(2, sweep(unmix, nothing))
    normal1 = (spread(scaling1, C2), spread(-mean1 * scaling1, C2))

    def unpool(k, carry):
        d_shift, d_gain = carry
        rows = step_rows(k)
        for pc in range(2):
            windows = row_windows(col_ref, pc, k)
            for pr in range(2):
                plane = pr * 2 + pc
                valid = inv_ref[plane, rows] > 0.0
                d_normal = windows[pr] - scale1 * dx_ref[plane, rows]
                d_normal = jnp.where(valid, d_normal, 0.0)
                back_ref[plane, rows] = d_normal
                normal = affine(x_ref[plane, rows], *normal1)
                d_shift = d_shift + fold(d_normal)
                d_gain = d_gain + fold(d_normal * normal)
        return (d_shift, d_gain)

    d_shift, d_gain = sweep(unpool, (nothing, nothing))
    add_up(1, d_shift)
    add_up(0, d_gain)
    mean_shift = by_image(d_shift * gain1) / count_two
    mean_gain = by_image(d_gain * gain1) / count_two
    back_gain1 = scaling1 * gain1
    back_mean1 = spread(-scaling1 * mean_shift, C2)
    back_normal1 = spread(scaling1 * mean_gain, C2)

    def unnorm(k, carry):
        rows = step_rows(k)
        for plane in range(4):
            normal = affine(x_ref[plane, rows], *normal1)
            back = affine(back_ref[plane, rows], back_gain1, back_mean1)
            back = back - scaled(normal, back_normal1)
            valid = inv_ref[plane, rows] > 0.0
            dx_ref[plane, rows] = jnp.where(valid, dx_ref[plane, rows] + back, 0.0)
        return carry

    sweep(unnorm, 0)

    def give_back(plane, here, spot, there):
        image_ref[spot, there] = dx_ref[plane, here]

    image_ref[...] = jnp.zeros(image_ref.shape, f32)
    each_image(bucket_of, pair, give_back)

    for spot in range(2 * STRIPS):
        target = strip_place(pair, spot, strip_count)
        for within in range(SR):
            rows = slice(within * CW, within * CW + CW)
            payload_ref[target, within] = image_ref[spot, rows].astype(bf16)

    def finish():
        copy = pltpu.make_async_copy(payload_ref, payload_hbm, sem)
        copy.start()
        vector_ref[...] = flat_ref[...]
        for n in range(3):
            vector_ref[n : n + 1] = jnp.sum(acc_ref[n], axis=0, keepdims=True)
        copy.wait()

    if pairs == 1:
        finish()
    else:
        pl.when(pair == pairs - 1)(finish)


def run_exit(place, buckets, state, back, flat, vec, strip_count):
    pairs = strip_count // 8
    payload = (strip_count, SR, CW, C2)
    make = pltpu.VMEM if pairs == 1 else jax.ShapeDtypeStruct
    plane_f32 = pltpu.VMEM((4, AREA, C2), f32)
    arrays = [*state, *back]
    if pairs == 1:
        arrays = held_in(pltpu.VMEM, *arrays)
    return pl.pallas_call(
        functools.partial(exit_kernel, pairs, strip_count),
        grid=() if pairs == 1 else (pairs,),
        in_specs=[SMEM] * 2
        + pair_specs(pairs, STATE + BACK, pl.Buffered(1))
        + whole_specs(pairs, [flat.shape, vec.shape]),
        out_specs=[HBM] + whole_specs(pairs, [flat.shape]),
        out_shape=[pltpu.HBM(payload, bf16), make(flat.shape, f32)],
        scratch_shapes=[
            pltpu.VMEM(payload, bf16),
            pltpu.VMEM((2 * STRIPS, STRIP_ROWS, C2), f32),
            pltpu.VMEM((4, AREA + 2 * LINE, C2), f32),
            plane_f32,
            plane_f32,
            pltpu.VMEM((3, 8, C2), f32),
            pltpu.SemaphoreType.DMA,
        ],
        compiler_params=roomy(8 if pairs == 1 else 40),
        name="exit",
    )(place, buckets, *arrays, flat, vec)


def dense_blocks(values):
    return jnp.concatenate([values[:, :HALF], values[:, HALF:]], axis=2).astype(bf16)


def pack_kernel(master_ref, dense_ref):
    dense_ref[...] = dense_blocks(master_ref[...])


def pack(master):
    owned = master.shape[0]
    return pl.pallas_call(
        pack_kernel,
        out_shape=jax.ShapeDtypeStruct((owned, HALF, 2 * BS), bf16),
        name="pack",
    )(master)


def pack_pieces_kernel(place_ref, master_hbm, pixel_hbm, *refs):
    out_refs, (wide_ref, master_ref, pixel_ref, sem) = refs[:-4], refs[-4:]
    owned = master_ref.shape[0]
    slots = pixel_ref.shape[2]
    copies = [pltpu.make_async_copy(pixel_hbm, pixel_ref, sem.at[0])]
    parts = [(0, owned // 2), (owned // 2, owned - owned // 2)]
    for n, part in enumerate(parts):
        copies.append(
            pltpu.make_async_copy(
                master_hbm.at[pl.ds(*part)], master_ref.at[pl.ds(*part)], sem.at[1 + n]
            )
        )
    for copy in copies:
        copy.start()
    copies[0].wait()

    def widen_row(row, carry):
        start = pl.multiple_of(row * CW * slots, 8)
        values = pixel_ref[row].astype(f32).reshape(CW * slots, C2)
        wide_ref[pl.ds(start, CW * slots)] = values
        return carry

    lax.fori_loop(0, SR, widen_row, 0)
    for k, ref in enumerate(out_refs):
        for other in range(2):
            slot = place_ref[0] ^ (2 * k + other)
            first = other * (ref.shape[0] - STRIP_ROWS)
            strip = wide_ref[pl.ds(slot, STRIP_ROWS, stride=slots)]
            ref[first : first + STRIP_ROWS] = strip.astype(bf16)
    for (first, count), copy in zip(parts, copies[1:]):
        copy.wait()
        dense = dense_blocks(master_ref[first : first + count]).reshape(count * HALF, 2 * BS)
        start = STRIP_ROWS + first * HALF
        for ref in out_refs[:3]:
            ref[start : start + count * HALF] = dense


def pack_pieces(place, master, pixels):
    slots = pixels.shape[2]
    rows = master.shape[0] * HALF
    shapes = [(rows + 2 * STRIP_ROWS, 2 * BS)] * 3 + [(2 * STRIP_ROWS, 2 * BS)]
    return pl.pallas_call(
        pack_pieces_kernel,
        in_specs=[SMEM] + [HBM] * 2,
        out_specs=[VMEM_BLOCK] * 4,
        out_shape=[pltpu.VMEM(shape, bf16) for shape in shapes],
        scratch_shapes=[
            pltpu.VMEM((STRIP_ROWS * slots, C2), f32),
            pltpu.VMEM(master.shape, f32),
            pltpu.VMEM(pixels.shape, bf16),
            pltpu.SemaphoreType.DMA((3,)),
        ],
        compiler_params=roomy(12),
        name="pack",
    )(place, *held_in(pltpu.HBM, master, pixels))


def fold_pair_kernel(near_ref, got_ref, own_ref, *part_refs):
    share = own_ref.shape[0]

    def one(n, carry):
        for k in range(len(part_refs) + 1):
            total = near_ref[k * share + n].astype(f32) + got_ref[k * share + n].astype(f32)
            if k == 0:
                own_ref[n] = total
            else:
                part_refs[k - 1][n] = total.astype(bf16)
        return carry

    lax.fori_loop(0, share, one, 0, unroll=4)


def fold_pair(near, got, groups):
    shape = ((near.shape[0] - 1) // groups,) + near.shape[1:]
    return pl.pallas_call(
        fold_pair_kernel,
        in_specs=[VMEM_BLOCK] * 2,
        out_specs=[VMEM_BLOCK] * groups,
        out_shape=[pltpu.VMEM(shape, f32)] + [pltpu.VMEM(shape, bf16)] * (groups - 1),
        compiler_params=roomy(4),
        name="fold_pair",
    )(*held_in(pltpu.VMEM, near, got))


def fold_tile_kernel(pieces, spot_ref, *refs):
    piece_refs, refs = refs[:pieces], refs[pieces:]
    vector_refs, refs = refs[:pieces], refs[pieces:]
    out_refs, sum_ref = refs[:-1], refs[-1]
    groups = len(out_refs)
    share = out_refs[0].shape[0]
    owned = piece_refs[0].shape[0]
    total = vector_refs[0][...]
    for ref in vector_refs[1:]:
        total = total + ref[...]
    for n in range(sum_ref.shape[0]):
        sum_ref[n] = jnp.zeros((HALF, 128), f32)
    for n in range(VEC_BLOCKS):
        sum_ref[n] = total[n * HALF : (n + 1) * HALF]

    def one(n, carry):
        for k, out_ref in enumerate(out_refs):
            number = lax.rem(spot_ref[0] + k, groups) * share + n
            block = jnp.minimum(number, owned - 1)
            total = piece_refs[0][block].astype(f32)
            for ref in piece_refs[1:]:
                total = total + ref[block].astype(f32)
            rest = sum_ref[jnp.maximum(number - owned, 0)]
            out_ref[n] = jnp.where(number < owned, total, rest).astype(out_ref.dtype)
        return carry

    lax.fori_loop(0, share, one, 0, unroll=share <= 16)


def fold_tile(spot, pieces, vectors, extra, groups):
    shape = ((pieces[0].shape[0] + extra) // groups,) + pieces[0].shape[1:]
    return pl.pallas_call(
        functools.partial(fold_tile_kernel, len(pieces)),
        in_specs=[SMEM] + [VMEM_BLOCK] * (len(pieces) + len(vectors)),
        out_specs=[VMEM_BLOCK] * groups,
        out_shape=[pltpu.VMEM(shape, f32)] + [pltpu.VMEM(shape, bf16)] * (groups - 1),
        scratch_shapes=[pltpu.VMEM((extra, HALF, 128), f32)],
        compiler_params=roomy(8),
        name="fold_tile",
    )(spot, *held_in(pltpu.VMEM, *pieces, *vectors))


def fold_batch_kernel(owned, vector_weight, spot_ref, *refs):
    part_refs, (total_ref, norm_ref) = refs[:-2], refs[-2:]
    share = total_ref.shape[0]
    square = jnp.zeros((8, 128), f32)
    for n in range(share):
        total = part_refs[0][n].astype(f32)
        for ref in part_refs[1:]:
            total = total + ref[n].astype(f32)
        total_ref[n] = total.astype(bf16)
        weight = jnp.where(spot_ref[0] * share + n < owned, 1.0, vector_weight)
        square = square + weight * fold(total * total)
    square = jnp.sum(jnp.sum(square, axis=1, keepdims=True), axis=0, keepdims=True)
    norm_ref[...] = jnp.broadcast_to(square[None], norm_ref.shape)


def fold_batch(spot, parts, owned, tile_count):
    count = tile_count * len(parts)
    return pl.pallas_call(
        functools.partial(fold_batch_kernel, owned, 1.0 / tile_count),
        in_specs=[SMEM] + [VMEM_BLOCK] * len(parts),
        out_specs=[VMEM_BLOCK] * 2,
        out_shape=[pltpu.VMEM(parts[0].shape, bf16), pltpu.VMEM((count, 1, 128), f32)],
        name="fold_batch",
    )(spot, *held_in(pltpu.VMEM, *parts))


def update_kernel(owned, groups, spot_ref, norm_ref, *refs):
    quarters, refs = refs[:groups], refs[groups:]
    stat_hbm, out_hbm, (vector_ref, clip_ref), refs = refs[:5], refs[5:10], refs[10:12], refs[12:]
    stat_refs, out_refs, (in_sem, out_sem) = refs[:5], refs[5:10], refs[10:]
    master_ref, left_stat_ref, right_stat_ref, left_root_ref, right_root_ref = stat_refs
    grad_ref, left_ref, right_ref, new_ref, copy_ref = out_refs
    share = quarters[0].shape[0]
    spans = spans_of(owned)

    def copies_of(sources, targets, sems):
        return [
            [
                pltpu.make_async_copy(
                    source.at[pl.ds(*span)], target.at[pl.ds(*span)], sems.at[5 * n + k]
                )
                for k, (source, target) in enumerate(zip(sources, targets))
            ]
            for n, span in enumerate(spans)
        ]

    copies_in = copies_of(stat_hbm, stat_refs, in_sem)
    copies_out = copies_of(out_refs, out_hbm, out_sem)
    for copies in copies_in:
        for copy in copies:
            copy.start()
    norm = jnp.sqrt(jnp.sum(norm_ref[...], axis=0))
    factor = jnp.minimum(1.0, clip_limit / norm)
    left_half = lax.broadcasted_iota(jnp.int32, (HALF, 128), 1) < BS

    def summed(number):
        source = number // share
        local = number - source * share
        turn = lax.rem(spot_ref[0] - source + groups, groups)
        value = quarters[0][local].astype(f32)
        for k in range(1, groups):
            value = jnp.where(turn == k, quarters[k][local].astype(f32), value)
        return value * factor

    def side_by_side(first, count):
        sides = []
        for n in range(first, first + count, 2):
            dense = summed(n)
            turned = pltpu.roll(dense, BS, 1)
            if n + 1 < first + count:
                second = summed(n + 1)
                top = jnp.where(left_half, dense, pltpu.roll(second, BS, 1))
                low = jnp.where(left_half, turned, second)
                side = jnp.concatenate([top, low], axis=0)
                grad_ref[n + 1] = pltpu.roll(side, BS, 1)[:, :BS]
            else:
                side = jnp.concatenate([dense, turned], axis=0)[:, :BS]
            grad_ref[n] = side[:, :BS]
            sides.append(side.astype(bf16))
        return jnp.concatenate(sides, axis=1)

    def diagonal_of(count):
        order = (count * BS, count * BS)
        return lax.broadcasted_iota(jnp.int32, order, 0) // BS == (
            lax.broadcasted_iota(jnp.int32, order, 1) // BS
        )

    clip_ref[...] = norm
    for n in range(vector_ref.shape[0]):
        vector_ref[n] = summed(owned + n)
    for (first, length), arriving, leaving in zip(spans, copies_in, copies_out):
        parts = [(n, min(4, first + length - n)) for n in range(first, first + length, 4)]
        wides = [side_by_side(*part) for part in parts]
        tall = [
            jnp.where(diagonal_of(count), jnp.concatenate([wide] * count, axis=0), 0.0)
            for (_, count), wide in zip(parts, wides)
        ]
        lefts = [product_nt(one, wide) for one, wide in zip(tall, wides)]
        rights = [product_tn(wide, wide) for wide in wides]
        for copy in arriving:
            copy.wait()
        stepped = []
        for (start, count), wide in zip(parts, wides):
            roots = left_root_ref[pl.ds(start, count)].reshape(count * BS, BS).astype(bf16)
            stepped.append(product(roots, wide))
        for (start, count), left, right in zip(parts, lefts, rights):
            here = pl.ds(start, count)
            left_ref[here] = 0.5 * left_stat_ref[here] + 0.5 * left.reshape(count, BS, BS)
            for n in range(count):
                at = n // 2 * 128
                block = right[n * BS : n * BS + BS, at : min(at + 128, count * BS)]
                if n % 2:
                    block = pltpu.roll(block, BS, 1)
                right_ref[start + n] = 0.5 * right_stat_ref[start + n] + 0.5 * block[:, :BS]
        for (start, count), value in zip(parts, stepped):
            here = pl.ds(start, count)
            value = jnp.where(diagonal_of(count), value, 0.0).astype(bf16)
            roots = right_root_ref[here].reshape(count * BS, BS).astype(bf16)
            value = product(value, roots).reshape(count, BS, BS)
            new = master_ref[here] - rate_matrix * value
            new_ref[here] = new
            copy_ref[here] = new.astype(bf16)
        for copy in leaving:
            copy.start()
    for leaving in copies_out:
        for copy in leaving:
            copy.wait()


def spans_of(owned):
    spans = []
    first = 0
    while first < owned:
        length = min(8 if first == 0 else 12, owned - first)
        spans.append((first, length))
        first += length
    return spans


def update(spot, norm, quarters, extra, *stats):
    shape = stats[0].shape
    groups = len(quarters)
    types = [f32] * 4 + [bf16]
    steps = len(spans_of(shape[0]))
    return pl.pallas_call(
        functools.partial(update_kernel, shape[0], groups),
        in_specs=[SMEM] + [VMEM_BLOCK] * (groups + 1) + [HBM] * 5,
        out_specs=[HBM] * 5 + [VMEM_BLOCK] * 2,
        out_shape=[pltpu.HBM(shape, kind) for kind in types]
        + [
            pltpu.VMEM((extra, HALF, 128), f32),
            pltpu.VMEM((1, 128), f32),
        ],
        scratch_shapes=[pltpu.VMEM(shape, f32)] * 5
        + [pltpu.VMEM(shape, kind) for kind in types]
        + [
            pltpu.SemaphoreType.DMA((5 * steps,)),
            pltpu.SemaphoreType.DMA((5 * steps,)),
        ],
        compiler_params=roomy(20),
        name="update",
    )(spot, *held_in(pltpu.VMEM, norm, *quarters), *held_in(pltpu.HBM, *stats))


def share_out(pieces, axis):
    return lax.all_to_all(pieces, axis, split_axis=0, concat_axis=0, tiled=True)


def swap(piece, distance):
    count = lax.axis_size("tile")
    return lax.ppermute(piece, "tile", [(i, i ^ distance) for i in range(count)])


def on_device(
    pixels,
    buckets,
    slot_owner_table,
    out_grad,
    master,
    left_stat,
    right_stat,
    left_root,
    right_root,
    vectors,
    moment,
):
    tile_count = lax.axis_size("tile")
    tile_place = lax.axis_index("tile")
    slot_count = pixels.shape[2]
    group_count = tile_count // STRIPS
    pairs = group_count // 2
    owned = master.shape[0]
    slots = owned * tile_count
    batch_count = lax.axis_size("batch")
    spot = lax.axis_index("batch").astype(jnp.int32).reshape(1)
    extra = extra_of(owned, batch_count)
    place = tile_place.astype(jnp.int32).reshape(1)
    paired = tile_count == 8
    numbers = jnp.arange(slots, dtype=jnp.int32)
    slot_of = jnp.sum(
        jnp.where(slot_owner_table[None, :] == numbers[:, None], numbers[None, :], 0), axis=1
    )
    if paired:
        owner = slot_of // owned
        apart = owner ^ tile_place
        apart = (apart & 1) * (tile_count // 2) + (apart >> 1)
        slot_of = slot_of + owned * (apart - owner)
    half = slots // 2
    near_place = jnp.where(slot_of < half, slot_of, half)
    far_place = jnp.where(slot_of < half, half, slot_of - half)
    vec = vectors.reshape(-1, 128)
    turned = lax.dynamic_index_in_dim(
        buckets.reshape(group_count, slot_count), tile_place, 1, keepdims=False
    ) >= 2
    flips = turned.reshape(-1, 1, 1, 1)
    goal = out_grad.reshape(2 * pairs, H3, W3, C3)
    goal = jnp.where(flips, goal.transpose(0, 2, 1, 3), goal)[:, :LINES]
    goal = goal.reshape(pairs, 2, LINES, W3, C3).transpose(0, 2, 3, 1, 4)
    goal = goal.reshape(pairs, LINES, 2 * W3, C3)
    goal = jnp.pad(goal, ((0, 0), (0, 0), (0, LINE - 2 * W3), (0, WIDE - C3)))
    goal = goal.reshape(pairs, AREA, WIDE)

    if paired:
        own, for_x, for_y, for_both = pack_pieces(
            place, master, pixels[0, 0].transpose(1, 2, 0, 3)
        )
        goal, vec, slot_of, near_place, far_place, for_both = lax.optimization_barrier(
            (goal, vec, slot_of, near_place, far_place, for_both)
        )
        from_x, from_y, strips_both = swap(for_x, 2), swap(for_y, 4), swap(for_both, 6)
        near_half = (owned + 1) // 2
        middle = STRIP_ROWS + near_half * HALF
        first_half = swap(from_x[STRIP_ROWS:middle], 4)
        second_half = swap(from_y[middle : STRIP_ROWS + owned * HALF], 2)
        mine = [own, from_x, from_y, strips_both, first_half, second_half]
        both = mine + [swap(piece, 1) for piece in mine]
        strips = both[:4] + both[6:10]
        pieces = [both[n] for n in (0, 1, 2, 4, 5, 6, 7, 8, 10, 11)]
        spans = [(STRIP_ROWS, owned)] * 3 + [(0, near_half), (0, owned - near_half)]
        spans = spans * 2
    else:
        pieces = [lax.all_gather(pack(master), "tile", axis=0, tiled=True).reshape(-1, 2 * BS)]
        spans = [(0, slots)]
        strips = share_out(pixels.reshape(tile_count, STRIP, C2), "tile")
        strips = [jnp.pad(strips, ((0, 0), (0, STRIP_ROWS - STRIP), (0, 0)))]

    weights = run_unpack(slot_of, pieces, spans)
    state = run_entry(place, buckets, strips, vec, tile_count)
    result, *back, near, far, flat = run_main(
        (near_place, far_place),
        place,
        buckets,
        state,
        goal,
        vec,
        weights,
        tile_count,
    )
    pixel_back, vector = run_exit(place, buckets, state, back, flat, vec, tile_count)
    if paired:
        own, *parts = fold_pair(near, swap(far, 1), tile_count // 2)
        pieces = [own] + [swap(part, 2 * k + 2) for k, part in enumerate(parts)]
        vector, _ = lax.optimization_barrier((vector, parts[0]))
        vector = vector + swap(vector, 1)
        vectors_in = [vector] + [swap(vector, 2 * k) for k in range(1, tile_count // 2)]
    else:
        outgoing = jnp.concatenate([near[:half], far[:half]], axis=0)
        pieces = list(share_out(outgoing.reshape(tile_count, owned, HALF, 128), "tile"))
        vectors_in = list(lax.all_gather(vector, "tile"))
    result, pieces[1] = lax.optimization_barrier((result, pieces[1]))
    result = result.reshape(pairs, LINES, LINE, WIDE)[:, :, : 2 * W3, :C3]
    result = result.reshape(pairs, LINES, W3, 2, C3).transpose(0, 3, 1, 2, 4)
    result = result.reshape(2 * pairs, LINES, W3, C3)
    result = jnp.pad(result, ((0, 0), (0, H3 - LINES), (0, 0), (0, 0)))
    result = jnp.where(flips, result.transpose(0, 2, 1, 3), result)
    result = result.reshape(out_grad.shape)
    result = with_layout_constraint(result, Layout(major_to_minor=(0, 1, 2, 4, 5, 3, 6)))
    result, vectors_in[0] = lax.optimization_barrier((result, vectors_in[0]))
    own, *parts = fold_tile(spot, pieces, vectors_in, extra, batch_count)
    pixel_back, parts[0] = lax.optimization_barrier((pixel_back, parts[0]))
    returned = share_out(pixel_back, "tile")
    parts = [
        lax.ppermute(part, "batch", [(i, (i + k + 1) % batch_count) for i in range(batch_count)])
        for k, part in enumerate(parts)
    ]
    quarter, norm = fold_batch(spot, [own] + parts, owned, tile_count)
    returned, norm = lax.optimization_barrier((returned, norm))
    norm = share_out(norm, ("batch", "tile"))
    returned = returned.astype(f32).reshape(pixels.shape)
    returned = with_layout_constraint(returned, Layout(major_to_minor=(0, 1, 3, 4, 2, 5)))
    returned, quarter = lax.optimization_barrier((returned, quarter))
    quarters = [quarter] + [
        lax.ppermute(quarter, "batch", [(i, (i + k) % batch_count) for i in range(batch_count)])
        for k in range(1, batch_count)
    ]
    block_grad, left_new, right_new, master_new, weight_copy, whole_vector, clip = update(
        spot, norm, quarters, extra, master, left_stat, right_stat, left_root, right_root
    )
    clip_norm = clip[0, 0]
    share = vectors.shape[0] // tile_count
    whole_vector = whole_vector.reshape(-1)
    vec_grad = lax.dynamic_slice_in_dim(whole_vector, tile_place * share, share, 0)
    vec_moment = moment + vec_grad * vec_grad
    own_vectors = lax.dynamic_slice_in_dim(vectors, tile_place * share, share, 0)
    vec_new = own_vectors - rate_vector * vec_grad / (jnp.sqrt(vec_moment) + eps_adagrad)
    return (
        result,
        returned,
        clip_norm,
        block_grad,
        left_new,
        right_new,
        master_new,
        weight_copy,
        vec_grad,
        vec_moment,
        vec_new,
    )


def solution(mesh):
    placed = (
        P("batch", "tile", None, None, None, None),
        P("batch"),
        P(),
        P("batch", "tile", None, None, None, None, None),
        P("tile", None, None),
        P("tile", None, None),
        P("tile", None, None),
        P("tile", None, None),
        P("tile", None, None),
        P(),
        P("tile"),
    )
    return jax.shard_map(
        on_device,
        mesh=mesh,
        in_specs=placed,
        out_specs=(
            P("batch", "tile", None, None, None, None, None),
            P("batch", "tile", None, None, None, None),
            P(),
            P("tile", None, None),
            P("tile", None, None),
            P("tile", None, None),
            P("tile", None, None),
            P("tile", None, None),
            P("tile"),
            P("tile"),
            P("tile"),
        ),
        check_vma=False,
    )
```

```python
import functools

import jax
import jax.numpy as jnp
from jax import lax
from jax.experimental import pallas as pl
from jax.experimental.layout import Layout, with_layout_constraint
from jax.experimental.pallas import tpu as pltpu
from jax.sharding import PartitionSpec as P

C2 = 128
HID2 = 512
C3 = 320
HID3 = 1280
CH = 36
CW = 36
STRIPS = 4
BS = 64
SR = CH // STRIPS
H3 = CH // 2
W3 = CW // 2
LONG = 7 * CH // 9
LINES = LONG // 2
WIDE = 384
LINE = 40
AREA = LINES * LINE
STEP = 2 * LINE
STEPS = AREA // STEP
HALF = BS // 2
STRIP = SR * CW
STRIP_ROWS = STRIP + -STRIP % 16

eps_norm = 1e-05
clip_limit = 1.0
rate_matrix = 0.3
rate_vector = 0.3
eps_adagrad = 1e-08
f32 = jnp.float32
bf16 = jnp.bfloat16

SHAPES = [(C2, HID2), (HID2, C2), (9 * C2, C3), (C3, HID3), (HID3, C3)]
USED = sum(rows // BS * (cols // BS) for rows, cols in SHAPES)
VEC_ROWS = (6 * C2 + HID2 + C2 + C3 + 6 * C3 + HID3 + C3) // 128


VEC_BLOCKS = -(-VEC_ROWS // HALF)


def extra_of(owned, groups):
    return VEC_BLOCKS + -(owned + VEC_BLOCKS) % groups


def product(left, right):
    return jnp.dot(left, right, preferred_element_type=f32)


def product_nt(left, right):
    return lax.dot_general(left, right, (((1,), (1,)), ((), ())), preferred_element_type=f32)


def product_tn(left, right):
    return lax.dot_general(left, right, (((0,), (0,)), ((), ())), preferred_element_type=f32)


def gelu_pair(values):
    bell = jnp.exp2(values * values * (-0.5 * 1.4426950408889634))
    step = pl.reciprocal(1.0 + (0.3275911 * 0.7071067811865476) * jnp.abs(values), approx=True)
    tail = step * (
        0.5 * 0.254829592
        + step
        * (
            0.5 * -0.284496736
            + step
            * (0.5 * 1.421413741 + step * (0.5 * -1.453152027 + step * (0.5 * 1.061405429)))
        )
    )
    tail = tail * bell
    share = jnp.where(values >= 0.0, 1.0 - tail, tail)
    return (values * share, share + values * (bell * 0.3989422804014327))


def fold(values):
    chans = values.shape[-1]
    return jnp.sum(values.reshape(-1, 8, chans), axis=0)


def by_image(total):
    total = total + pltpu.roll(total, 4, 0)
    total = total + pltpu.roll(total, 2, 0)
    return jnp.sum(total, axis=1, keepdims=True)


def line(pattern):
    return jnp.concatenate([pattern] * (LINE // 8), axis=0)


def spread(pattern, chans):
    return jnp.broadcast_to(pattern, (8, chans))


def affine(values, factor, shift):
    tiles = values.reshape(-1, 8, values.shape[-1])
    return (tiles * factor + shift).reshape(values.shape)


def scaled(values, factor):
    tiles = values.reshape(-1, 8, values.shape[-1])
    return (tiles * factor).reshape(values.shape)


def from_left(values):
    return pltpu.roll(values, 2, 0)


def from_right(values):
    return pltpu.roll(values, values.shape[0] - 2, 0)


def rounded(values):
    return values.astype(bf16).astype(f32)


def widen(values):
    return jnp.concatenate([values] * (WIDE // 128), axis=-1)


def norm_terms(total, square, count):
    mean = by_image(total) / count
    scaling = lax.rsqrt(by_image(square) / count - mean * mean + eps_norm)
    return (mean, scaling)


def sweep(visit, start):
    return lax.fori_loop(0, STEPS, visit, start, unroll=True)


def step_rows(k, lines=0):
    start = k * STEP + lines * LINE
    return pl.ds(start if isinstance(k, int) else pl.multiple_of(start, LINE), STEP)


def held_in(space, *arrays):
    return [pltpu.with_memory_space_constraint(array, space) for array in arrays]


VMEM_BLOCK = pl.BlockSpec(memory_space=pltpu.VMEM)
HBM = pl.BlockSpec(memory_space=pltpu.HBM)
SMEM = pl.BlockSpec(memory_space=pltpu.SMEM)


def roomy(mebibytes):
    return pltpu.CompilerParams(vmem_limit_bytes=mebibytes * 1024 * 1024)


def image_shape(bucket_of, pair, image):
    bucket = bucket_of(2 * pair + image)
    plain = jnp.where(bucket == 0, 5 * CH // 9, 7 * CH // 9)
    across = jnp.where(bucket == 0, CW, 7 * CW // 9)
    turned = (bucket >= 2).astype(jnp.int32)
    return (
        jnp.where(turned > 0, 5 * CW // 9, plain),
        jnp.where(turned > 0, CH, across),
        turned,
    )


def bucket_reader(place_ref, bucket_ref, strip_count):
    return lambda group: bucket_ref[group * strip_count + place_ref[0]]


class Geometry:
    def __init__(self, bucket_of, pair):
        parity = lax.broadcasted_iota(jnp.int32, (8, 128), 0) % 2
        even, odd = (image_shape(bucket_of, pair, image) for image in range(2))
        high, broad, turned = (jnp.where(parity == 0, a, b) for a, b in zip(even, odd))
        self.high = high
        self.count_two = (high * broad * C2).astype(f32)[:, :1]
        self.high3 = (high + 1) // 2
        broad3 = (broad + 1) // 2
        self.count_three = (self.high3 * broad3 * C3).astype(f32)[:, :1]
        place = lax.broadcasted_iota(jnp.int32, (LINE, 128), 0) // 2
        inside = lax.broadcasted_iota(jnp.int32, (LINE, 128), 0) < 2 * W3
        self.reach = []
        self.col_share = []
        for pc in range(2):
            column = 2 * place + pc
            self.reach.append(jnp.where(inside & (column < line(broad)), line(high), 0))
            edge = (column == 0) | (column == line(broad) - 1)
            self.col_share.append(jnp.where(edge, 0.5, 1.0 / 3.0))
        self.reach3 = jnp.where(inside & (place < line(broad3)), line(self.high3), 0)
        edge3 = (place == 0) | (place == line(broad3) - 1)
        self.col_share3 = jnp.where(edge3, 0.5, 1.0 / 3.0)
        self.flipped = jnp.concatenate([turned] * (STEP // 8), axis=0) > 0

    def share(self, plane, k):
        pr, pc = plane // 2, plane % 2
        return self.lines(4 * k + pr, 2, self.reach[pc], self.col_share[pc], self.high)

    def share3(self, k):
        return self.lines(2 * k, 1, self.reach3, self.col_share3, self.high3)

    def lines(self, row, stride, reach, col_share, height):
        parts = []
        for n in range(2):
            here = row + stride * n
            row_share = jnp.where((here == 0) | (here == height - 1), 0.5, 1.0 / 3.0)
            parts.append(jnp.where(here < reach, line(row_share) * col_share, 0.0))
        return jnp.concatenate(parts, axis=0)


def strip_place(pair, spot, strip_count):
    return lax.rem(pair * 8 + strip_count - 2 + spot, strip_count)


def each_image(bucket_of, pair, visit):
    for image in range(2):
        way = image_shape(bucket_of, pair, image)[2]

        @pl.when(way == 0)
        def _():
            def one(r, carry):
                for plane in range(4):
                    row = 2 * r + plane // 2
                    strip = row // SR
                    there = pl.ds((row - strip * SR) * CW + plane % 2, W3, stride=2)
                    here = pl.ds(r * LINE + image, W3, stride=2)
                    visit(plane, here, image * STRIPS + strip, there)
                return carry

            lax.fori_loop(0, LINES, one, 0)

        @pl.when(way == 1)
        def _():
            def one(r, carry):
                for plane in range(4):
                    for strip in range(STRIPS):
                        first = (plane % 2 + strip * SR) % 2
                        count = (SR - first + 1) // 2
                        done = (strip * SR + first) // 2
                        column = 2 * r + plane // 2
                        there = pl.ds(first * CW + column, count, stride=2 * CW)
                        here = pl.ds(r * LINE + image + 2 * done, count, stride=2)
                        visit(plane, here, image * STRIPS + strip, there)
                return carry

            lax.fori_loop(0, LINES, one, 0)


def row_windows(col_ref, pc, k):
    both = col_ref[pc, step_rows(k, 1)] + col_ref[2 + pc, step_rows(k, 1)]
    return (both + col_ref[2 + pc, step_rows(k)], both + col_ref[pc, step_rows(k, 2)])


def put_col_windows(col_ref, pr, k, even, odd):
    both = even + odd
    col_ref[pr * 2, step_rows(k, 1)] = both + from_left(odd)
    col_ref[pr * 2 + 1, step_rows(k, 1)] = both + from_right(even)


def clear_edges(col_ref):
    zero_line = jnp.zeros((LINE, C2), f32)
    for plane in range(4):
        col_ref[plane, 0:LINE] = zero_line
        col_ref[plane, AREA + LINE : AREA + 2 * LINE] = zero_line


def entry_kernel(pairs, strip_count, piece_count, place_ref, bucket_ref, vec_ref, *refs):
    piece_refs, refs = refs[:piece_count], refs[piece_count:]
    x_out, inv_out, pool_out, mix_out, stat_out, image_ref, col_ref = refs
    pair = pl.program_id(0) if pairs > 1 else 0
    x_ref, inv_ref, pool_ref, mix_ref = (ref.at[0] for ref in (x_out, inv_out, pool_out, mix_out))
    bucket_of = bucket_reader(place_ref, bucket_ref, strip_count)
    shape = Geometry(bucket_of, pair)
    gain1, bias1, scale1 = (vec_ref[n : n + 1] for n in range(3))
    clear_edges(col_ref)
    if piece_count > 1:
        half = piece_count // 2
        for n, ref in enumerate(piece_refs):
            source = place_ref[0] ^ (n // half + 2 * (n % half))
            spot = lax.rem(source + 2, 2 * STRIPS)
            first = 0 if n < half else ref.shape[0] - STRIP_ROWS
            image_ref[spot] = ref[first : first + STRIP_ROWS].astype(f32)
    else:
        for spot in range(2 * STRIPS):
            source = strip_place(pair, spot, strip_count)
            image_ref[spot] = piece_refs[0][source].astype(f32)

    def take_in(plane, here, spot, there):
        x_ref[plane, here] = image_ref[spot, there]

    each_image(bucket_of, pair, take_in)

    def arrange(k, carry):
        total, square = carry
        rows = step_rows(k)
        for plane in range(4):
            share = shape.share(plane, k)
            inv_ref[plane, rows] = share
            values = jnp.where(share > 0.0, x_ref[plane, rows], 0.0)
            x_ref[plane, rows] = values
            total = total + fold(values)
            square = square + fold(values * values)
        return (total, square)

    nothing = jnp.zeros((8, C2), f32)
    total, square = sweep(arrange, (nothing, nothing))
    mean1, scaling1 = norm_terms(total, square, shape.count_two)
    factor1 = scaling1 * gain1
    shift1 = bias1 - mean1 * scaling1 * gain1

    def window_cols(k, carry):
        rows = step_rows(k)
        for pr in range(2):
            masked = []
            for pc in range(2):
                plane = pr * 2 + pc
                normal = rounded(affine(x_ref[plane, rows], factor1, shift1))
                masked.append(jnp.where(inv_ref[plane, rows] > 0.0, normal, 0.0))
            put_col_windows(col_ref, pr, k, *masked)
        return carry

    sweep(window_cols, 0)

    def mix(k, carry):
        total, square = carry
        rows = step_rows(k)
        for pc in range(2):
            windows = row_windows(col_ref, pc, k)
            for pr in range(2):
                plane = pr * 2 + pc
                values = x_ref[plane, rows]
                share = inv_ref[plane, rows]
                pooled = windows[pr] * share - rounded(affine(values, factor1, shift1))
                pooled = jnp.where(share > 0.0, pooled, 0.0)
                mixed = values + scale1 * pooled
                pool_ref[plane, rows] = pooled
                mix_ref[plane, rows] = mixed
                total = total + fold(mixed)
                square = square + fold(mixed * mixed)
        return (total, square)

    total, square = sweep(mix, (nothing, nothing))
    mean2, scaling2 = norm_terms(total, square, shape.count_two)
    for n, value in enumerate((mean1, scaling1, mean2, scaling2)):
        stat_out[0, n] = spread(value, 128)


def pair_specs(pairs, shapes, mode=None):
    if pairs == 1:
        return [VMEM_BLOCK] * len(shapes)
    return [
        pl.BlockSpec(
            (1,) + shape, lambda t, rank=len(shape): (t,) + (0,) * rank, pipeline_mode=mode
        )
        for shape in shapes
    ]


def whole_specs(pairs, shapes):
    if pairs == 1:
        return [VMEM_BLOCK] * len(shapes)
    return [
        pl.BlockSpec(
            shape,
            lambda t, rank=len(shape): (0,) * rank,
            pipeline_mode=pl.Buffered(1),
        )
        for shape in shapes
    ]


def pair_arrays(pairs, shapes, kinds):
    make = pltpu.VMEM if pairs == 1 else jax.ShapeDtypeStruct
    return [make((pairs,) + shape, kind) for shape, kind in zip(shapes, kinds)]


STATE = [(4, AREA, C2)] * 4 + [(4, 8, 128)]
BACK = [(4, AREA, C2)] * 2 + [(2, 8, 128)]


def run_entry(place, buckets, pieces, vec, strip_count):
    pairs = strip_count // 8
    if pairs == 1:
        pieces = held_in(pltpu.VMEM, *pieces)
    return pl.pallas_call(
        functools.partial(entry_kernel, pairs, strip_count, len(pieces)),
        grid=() if pairs == 1 else (pairs,),
        in_specs=[SMEM] * 2 + whole_specs(pairs, [array.shape for array in (vec, *pieces)]),
        out_specs=pair_specs(pairs, STATE),
        out_shape=pair_arrays(pairs, STATE, [f32] * 5),
        scratch_shapes=[
            pltpu.VMEM((2 * STRIPS, STRIP_ROWS, C2), f32),
            pltpu.VMEM((4, AREA + 2 * LINE, C2), f32),
        ],
        compiler_params=roomy(6 if pairs == 1 else 40),
        name="entry",
    )(place, buckets, vec, *pieces)


WEIGHTS = [(C2, HID2), (HID2, C2), (9 * C2, WIDE), (WIDE, HID3), (HID3, WIDE)]


def unpack_kernel(spans, slot_ref, *refs):
    piece_refs, refs = refs[: len(spans)], refs[len(spans) :]
    weights, gathered_ref = refs[:-1], refs[-1]
    done = 0
    for ref, (first, count) in zip(piece_refs, spans):
        blocks = ref[first : first + count * HALF].reshape(count, HALF, 128)
        gathered_ref[done : done + count] = blocks
        done += count
    left_half = lax.broadcasted_iota(jnp.int32, (HALF, 128), 1) < BS
    offset = 0
    for (rows, cols), ref in zip(SHAPES, weights):
        wide = cols // BS
        for rb in range(rows // BS):
            for cb in range(0, wide, 2):
                number = offset + rb * wide + cb
                first = gathered_ref[slot_ref[number]]
                turned = pltpu.roll(first, BS, 1)
                if cb + 1 < wide:
                    second = gathered_ref[slot_ref[number + 1]]
                    top = jnp.where(left_half, first, pltpu.roll(second, BS, 1))
                    low = jnp.where(left_half, turned, second)
                else:
                    top = jnp.where(left_half, first, 0.0)
                    low = jnp.where(left_half, turned, 0.0)
                place = slice(cb * BS, cb * BS + 128)
                ref[rb * BS : rb * BS + HALF, place] = top
                ref[rb * BS + HALF : rb * BS + BS, place] = low
        offset += rows // BS * wide
    weights[3][C3:, :] = jnp.zeros((WIDE - C3, HID3), bf16)


def run_unpack(slot_of, pieces, spans):
    slots = slot_of.shape[0]
    return pl.pallas_call(
        functools.partial(unpack_kernel, spans),
        in_specs=[SMEM] + [VMEM_BLOCK] * len(pieces),
        out_specs=[VMEM_BLOCK] * 5,
        out_shape=[pltpu.VMEM(shape, bf16) for shape in WEIGHTS],
        scratch_shapes=[pltpu.VMEM((slots, HALF, 128), bf16)],
        compiler_params=roomy(6),
        name="unpack",
    )(slot_of, *held_in(pltpu.VMEM, *pieces))


def main_kernel(
    pairs,
    strip_count,
    slots,
    near_place,
    far_place,
    place_ref,
    bucket_ref,
    inv_in,
    mix_in,
    stat_in,
    goal_ref,
    vec_ref,
    w1_ref,
    w2_ref,
    we_ref,
    w3_ref,
    w4_ref,
    result_ref,
    zed_out,
    dx_out,
    mean_out,
    near_ref,
    far_ref,
    flat_ref,
    zed_ref,
    hid_ref,
    u_ref,
    g_ref,
    h_ref,
    dy_ref,
    patch_ref,
    dpatch_ref,
    inv3_ref,
    e_ref,
    col3_ref,
    pool3_ref,
    mix3_ref,
    dx3_ref,
    hid3_ref,
    dhid3_ref,
    u3_ref,
    g3_ref,
    h3_ref,
    dy3_ref,
    dpre_ref,
    gw1_ref,
    gw2_ref,
    gwe_ref,
    gw3_ref,
    gw4_ref,
    acc_two,
    acc_hid_two,
    acc_three,
    acc_hid_three,
):
    pair = pl.program_id(0) if pairs > 1 else 0
    grads = [gw1_ref, gw2_ref, gwe_ref, gw3_ref, gw4_ref]
    inv_ref, mix_ref, stat_ref = (ref.at[0] for ref in (inv_in, mix_in, stat_in))
    back_ref, dx_ref = zed_out.at[0], dx_out.at[0]
    left_half = lax.broadcasted_iota(jnp.int32, (HALF, 128), 1) < BS

    def at_pair(number, act):
        if pairs == 1:
            act()
        else:
            pl.when(pair == number)(act)

    def begin():
        acc_two[...] = jnp.zeros(acc_two.shape, f32)
        acc_hid_two[...] = jnp.zeros(acc_hid_two.shape, f32)
        acc_three[...] = jnp.zeros(acc_three.shape, f32)
        acc_hid_three[...] = jnp.zeros(acc_hid_three.shape, f32)

    at_pair(0, begin)
    shape = Geometry(bucket_reader(place_ref, bucket_ref, strip_count), pair)
    count_two, count_three, flipped = shape.count_two, shape.count_three, shape.flipped
    nothing = jnp.zeros((8, C2), f32)
    nothing3 = jnp.zeros((8, WIDE), f32)

    def vector_row(at, length):
        first, shift = at // 128, at % 128
        count = -(-(shift + length) // 128)
        row = jnp.concatenate([vec_ref[first + n : first + n + 1] for n in range(count)], axis=1)
        if shift:
            row = pltpu.roll(jnp.broadcast_to(row, (8, count * 128)), count * 128 - shift, 1)[:1]
        return row

    def wide_row(at):
        lane = lax.broadcasted_iota(jnp.int32, (1, WIDE), 1)
        return jnp.where(lane < C3, vector_row(at, C3)[:, :WIDE], 0.0)

    gain2, bias2, scale2 = (vec_ref[n : n + 1] for n in range(3, 6))
    hid_bias = vector_row(6 * C2, HID2)
    out_bias = vector_row(6 * C2 + HID2, C2)
    two = 7 * C2 + HID2
    embed_bias, gain3, bias3, scale3 = (wide_row(two + n * C3) for n in range(4))
    gain4, bias4, scale4 = (wide_row(two + n * C3) for n in range(4, 7))
    hid_bias3 = vector_row(two + 7 * C3, HID3)[:, :HID3]
    out_bias3 = wide_row(two + 7 * C3 + HID3)
    mean2, scaling2 = stat_ref[2], stat_ref[3]
    factor2 = scaling2 * gain2
    shift2 = bias2 - mean2 * scaling2 * gain2
    for plane in range(4):
        zed_ref[plane, 0:LINE] = jnp.zeros((LINE, C2), f32)
    col3_ref[0:LINE] = jnp.zeros((LINE, WIDE), f32)
    col3_ref[AREA + LINE : AREA + 2 * LINE] = jnp.zeros((LINE, WIDE), f32)

    def put_block(number, block):
        near_ref[near_place[number]] = block
        far_ref[far_place[number]] = block

    def pack_blocks(matrices):
        offsets = [0]
        for rows, cols in SHAPES:
            offsets.append(offsets[-1] + rows // BS * (cols // BS))
        for which in matrices:
            (rows, cols), ref = SHAPES[which], grads[which]
            wide = cols // BS
            for rb in range(rows // BS):
                for cb in range(0, wide, 2):
                    number = offsets[which] + rb * wide + cb
                    at = slice(cb * BS, cb * BS + 128)
                    top = ref[rb * BS : rb * BS + HALF, at].astype(bf16)
                    low = ref[rb * BS + HALF : rb * BS + BS, at].astype(bf16)
                    put_block(number, jnp.where(left_half, top, pltpu.roll(low, BS, 1)))
                    if cb + 1 < wide:
                        put_block(number + 1, jnp.where(left_half, pltpu.roll(top, BS, 1), low))

    def plane_rows(plane):
        return slice(plane * AREA, plane * AREA + AREA)

    def begin_plane(plane):
        low = affine(mix_ref[plane], factor2, shift2).astype(bf16)
        h_ref[plane_rows(plane)] = low
        hid_ref[plane % 2] = product(low, w1_ref[...])

    begin_plane(0)
    for plane in range(4):
        if plane < 3:
            begin_plane(plane + 1)
        for k in range(STEPS):
            rows = step_rows(k)
            flat = slice(plane * AREA + k * STEP, plane * AREA + k * STEP + STEP)
            for at in range(0, HID2, 128):
                lanes = slice(at, at + 128)
                active, slope = gelu_pair(hid_ref[plane % 2, rows, lanes] + hid_bias[:, lanes])
                u_ref[flat, lanes] = active.astype(bf16)
                g_ref[flat, lanes] = slope.astype(bf16)
        out = product(u_ref[plane_rows(plane)], w2_ref[...]) + out_bias
        zed = jnp.where(inv_ref[plane] > 0.0, mix_ref[plane] + scale2 * out, 0.0)
        zed_ref[plane, LINE : LINE + AREA] = rounded(zed)

    def patches(k, carry):
        rows = step_rows(k)
        taps = []
        for ky in range(3):
            pr = (0 if ky == 1 else 1) * 2
            source = step_rows(k, 0 if ky == 0 else 1)
            even = zed_ref[pr, source]
            odd = zed_ref[pr + 1, source]
            taps.append((from_left(odd), even, odd))
        for ky in range(3):
            for kx in range(3):
                at = (3 * ky + kx) * C2
                tap = taps[ky][kx]
                if ky != kx:
                    tap = jnp.where(flipped, taps[kx][ky], tap)
                patch_ref[rows, at : at + C2] = tap.astype(bf16)
        return carry

    sweep(patches, 0)
    e_ref[...] = product(patch_ref[...], we_ref[...])

    def embed(k, carry):
        total, square = carry
        rows = step_rows(k)
        share = shape.share3(k)
        inv3_ref[rows] = share
        out = jnp.where(widen(share) > 0.0, e_ref[rows] + embed_bias, 0.0)
        e_ref[rows] = out
        return (total + fold(out), square + fold(out * out))

    total, square = sweep(embed, (nothing3, nothing3))
    mean3, scaling3 = norm_terms(total, square, count_three)
    factor3 = scaling3 * gain3
    shift3 = bias3 - mean3 * scaling3 * gain3

    def window_cols3(k, carry):
        rows = step_rows(k)
        normal = rounded(affine(e_ref[rows], factor3, shift3))
        masked = jnp.where(widen(inv3_ref[rows]) > 0.0, normal, 0.0)
        col3_ref[step_rows(k, 1)] = masked + from_left(masked) + from_right(masked)
        return carry

    sweep(window_cols3, 0)

    def row_windows3(k):
        return col3_ref[step_rows(k)] + col3_ref[step_rows(k, 1)] + col3_ref[step_rows(k, 2)]

    def mix3(k, carry):
        total, square = carry
        rows = step_rows(k)
        values = e_ref[rows]
        share = widen(inv3_ref[rows])
        pooled = row_windows3(k) * share - rounded(affine(values, factor3, shift3))
        pooled = jnp.where(share > 0.0, pooled, 0.0)
        mixed = values + scale3 * pooled
        pool3_ref[rows] = pooled
        mix3_ref[rows] = mixed
        return (total + fold(mixed), square + fold(mixed * mixed))

    total, square = sweep(mix3, (nothing3, nothing3))
    mean4, scaling4 = norm_terms(total, square, count_three)
    factor4 = scaling4 * gain4
    shift4 = bias4 - mean4 * scaling4 * gain4
    normal4 = (spread(scaling4, WIDE), spread(-mean4 * scaling4, WIDE))

    def prepare3(k, d_bias):
        rows = step_rows(k)
        h3_ref[rows] = affine(mix3_ref[rows], factor4, shift4).astype(bf16)
        goal = goal_ref[0, rows].astype(f32)
        goal = jnp.where(widen(inv3_ref[rows]) > 0.0, goal, 0.0)
        low_goal = (scale4 * goal).astype(bf16)
        dy3_ref[rows] = low_goal
        return d_bias + fold(low_goal.astype(f32))

    acc_three[7] += sweep(prepare3, nothing3)

    def keep(ref, value, place=slice(None)):
        if pairs == 1:
            ref[place] = value.astype(ref.dtype)
        else:

            @pl.when(pair == 0)
            def _():
                ref[place] = value

            @pl.when(pair > 0)
            def _():
                ref[place] += value

    def begin_chunk(at):
        lanes = slice(at, at + 256)
        hid3_ref[:, lanes] = product(h3_ref[...], w3_ref[:, lanes])
        dhid3_ref[:, lanes] = product_nt(dy3_ref[...], w4_ref[lanes])

    begin_chunk(0)
    for at in range(0, HID3, 256):
        if at + 256 < HID3:
            begin_chunk(at + 256)
        for lane in (at, at + 128):
            lanes = slice(lane, lane + 128)
            total = nothing
            for k in range(STEPS):
                rows = step_rows(k)
                active, slope = gelu_pair(hid3_ref[rows, lanes] + hid_bias3[:, lanes])
                u3_ref[rows, lanes] = active.astype(bf16)
                low = (slope * dhid3_ref[rows, lanes]).astype(bf16)
                g3_ref[rows, lanes] = low
                total = total + fold(low.astype(f32))
            acc_hid_three[:, lanes] += total
        lanes = slice(at, at + 256)
        out = product(u3_ref[:, lanes], w4_ref[lanes])
        d_low = product_nt(g3_ref[:, lanes], w3_ref[:, lanes])
        result_ref[0] = out if at == 0 else result_ref[0] + out
        dx3_ref[...] = d_low if at == 0 else dx3_ref[...] + d_low
        keep(gw3_ref, product_tn(h3_ref[...], g3_ref[:, lanes]), (slice(None), lanes))
        keep(gw4_ref, product_tn(u3_ref[:, lanes], dy3_ref[...]), lanes)

    def finish3(k, carry):
        d_scale, d_shift, d_gain = carry
        rows = step_rows(k)
        valid = widen(inv3_ref[rows]) > 0.0
        mixed = mix3_ref[rows]
        out = jnp.where(valid, result_ref[0, rows] + out_bias3, 0.0)
        result_ref[0, rows] = mixed + scale4 * out
        d_scale = d_scale + fold(out * goal_ref[0, rows].astype(f32))
        d_low = dx3_ref[rows]
        normal = affine(mixed, *normal4)
        return (d_scale, d_shift + fold(d_low), d_gain + fold(d_low * normal))

    d_scale, d_shift, d_gain = sweep(finish3, (nothing3, nothing3, nothing3))
    acc_three[6] += d_scale
    acc_three[5] += d_shift
    acc_three[4] += d_gain
    mean_shift = by_image(d_shift * gain4) / count_three
    mean_gain = by_image(d_gain * gain4) / count_three
    back_gain4 = scaling4 * gain4
    back_mean4 = spread(-scaling4 * mean_shift, WIDE)
    back_normal4 = spread(scaling4 * mean_gain, WIDE)

    def unmix3(k, d_scale):
        rows = step_rows(k)
        share = widen(inv3_ref[rows])
        valid = share > 0.0
        normal = affine(mix3_ref[rows], *normal4)
        back = affine(dx3_ref[rows], back_gain4, back_mean4) - scaled(normal, back_normal4)
        d_mixed = jnp.where(valid, back + goal_ref[0, rows].astype(f32), 0.0)
        dx3_ref[rows] = d_mixed
        d_scale = d_scale + fold(pool3_ref[rows] * d_mixed)
        weighted = scale3 * d_mixed * share
        col3_ref[step_rows(k, 1)] = weighted + from_left(weighted) + from_right(weighted)
        return d_scale

    acc_three[3] += sweep(unmix3, nothing3)
    normal3 = (spread(scaling3, WIDE), spread(-mean3 * scaling3, WIDE))

    def unpool3(k, carry):
        d_shift, d_gain = carry
        rows = step_rows(k)
        valid = widen(inv3_ref[rows]) > 0.0
        d_normal = jnp.where(valid, row_windows3(k) - scale3 * dx3_ref[rows], 0.0)
        pool3_ref[rows] = d_normal
        normal = affine(e_ref[rows], *normal3)
        return (d_shift + fold(d_normal), d_gain + fold(d_normal * normal))

    d_shift, d_gain = sweep(unpool3, (nothing3, nothing3))
    acc_three[2] += d_shift
    acc_three[1] += d_gain
    mean_shift = by_image(d_shift * gain3) / count_three
    mean_gain = by_image(d_gain * gain3) / count_three
    back_gain3 = scaling3 * gain3
    back_mean3 = spread(-scaling3 * mean_shift, WIDE)
    back_normal3 = spread(scaling3 * mean_gain, WIDE)

    def unnorm3(k, d_bias):
        rows = step_rows(k)
        valid = widen(inv3_ref[rows]) > 0.0
        normal = affine(e_ref[rows], *normal3)
        back = affine(pool3_ref[rows], back_gain3, back_mean3) - scaled(normal, back_normal3)
        low = jnp.where(valid, dx3_ref[rows] + back, 0.0).astype(bf16)
        dpre_ref[rows] = low
        return d_bias + fold(low.astype(f32))

    acc_three[0] += sweep(unnorm3, nothing3)
    keep(gwe_ref, product_tn(patch_ref[...], dpre_ref[...]))
    dpatch_ref[0:AREA] = product_nt(dpre_ref[...], we_ref[...])
    dpatch_ref[AREA : AREA + LINE] = jnp.zeros((LINE, 9 * C2), f32)

    def gather_back(k, carry):
        rows = step_rows(k)

        def tap(ky, kx, source):
            at = (3 * ky + kx) * C2
            value = dpatch_ref[source, at : at + C2]
            if ky != kx:
                at = (3 * kx + ky) * C2
                value = jnp.where(flipped, dpatch_ref[source, at : at + C2], value)
            return value

        sources = []
        for ky in range(3):
            source = step_rows(k, 1 if ky == 0 else 0)
            sources.append(
                (tap(ky, 1, source), tap(ky, 2, source) + from_right(tap(ky, 0, source)))
            )
        for pc in range(2):
            for pr, value in ((0, sources[1][pc]), (1, sources[2][pc] + sources[0][pc])):
                plane = pr * 2 + pc
                valid = inv_ref[plane, rows] > 0.0
                back_ref[plane, rows] = jnp.where(valid, rounded(value), 0.0)
        return carry

    sweep(gather_back, 0)

    if pairs == 1:
        pack_blocks(range(2, 5))

    normal2 = (spread(scaling2, C2), spread(-mean2 * scaling2, C2))

    def begin_back(plane):
        low_goal = (scale2 * back_ref[plane]).astype(bf16)
        dy_ref[plane_rows(plane)] = low_goal
        hid_ref[plane % 2] = product_nt(low_goal, w2_ref[...])
        return fold(low_goal.astype(f32))

    d_out_bias = begin_back(0)
    d_shift, d_gain = nothing, nothing
    sums = [nothing] * (HID2 // 128)
    new_gw1, new_gw2 = None, None
    for plane in range(4):
        if plane < 3:
            d_out_bias = d_out_bias + begin_back(plane + 1)
        for k in range(STEPS):
            rows = step_rows(k)
            part = slice(plane * AREA + k * STEP, plane * AREA + k * STEP + STEP)
            for n, at in enumerate(range(0, HID2, 128)):
                lanes = slice(at, at + 128)
                low = g_ref[part, lanes].astype(f32) * hid_ref[plane % 2, rows, lanes]
                low = low.astype(bf16)
                g_ref[part, lanes] = low
                sums[n] = sums[n] + fold(low.astype(f32))
        flat = plane_rows(plane)
        d_low = product_nt(g_ref[flat], w1_ref[...])
        dx_ref[plane] = d_low
        d_shift = d_shift + fold(d_low)
        d_gain = d_gain + fold(d_low * affine(mix_ref[plane], *normal2))
        part_gw1 = product_tn(h_ref[flat], g_ref[flat])
        part_gw2 = product_tn(dy_ref[flat], u_ref[flat])
        new_gw1 = part_gw1 if plane == 0 else new_gw1 + part_gw1
        new_gw2 = part_gw2 if plane == 0 else new_gw2 + part_gw2
    new_gw2 = new_gw2.T
    for n, value in enumerate(sums):
        acc_hid_two[:, n * 128 : n * 128 + 128] += value
    acc_two[6] += d_out_bias
    acc_two[4] += d_shift
    acc_two[3] += d_gain
    mean_out[0, 0] = spread(by_image(d_shift * gain2) / count_two, 128)
    mean_out[0, 1] = spread(by_image(d_gain * gain2) / count_two, 128)
    keep(gw1_ref, new_gw1)
    keep(gw2_ref, new_gw2)
    d_scale = fold(w2_ref[...].astype(f32) * new_gw2) + out_bias * d_out_bias
    acc_two[5] += d_scale / scale2

    def finish():
        if pairs > 1:
            pack_blocks(range(5))
        else:
            pack_blocks(range(2))

        def filler(number, carry):
            put_block(number, jnp.zeros((HALF, 128), bf16))
            return carry

        lax.fori_loop(USED, slots, filler, 0)

        flat_ref[...] = jnp.zeros(flat_ref.shape, f32)

        def put(at, total, length):
            if at % 128:
                room = jnp.zeros((8, 128), f32)
                if total.shape[1] < length + BS:
                    total = jnp.concatenate([total, room], axis=1)
                total = pltpu.roll(total, BS, 1)
            whole = jnp.sum(total, axis=0, keepdims=True)
            done = -(at % 128)
            row = at // 128
            lane = 0
            while done < length:
                first = max(0, -done)
                last = min(128, length - done)
                flat_ref[row : row + 1, first:last] = whole[:, lane + first : lane + last]
                done += 128
                lane += 128
                row += 1

        at = 3 * C2
        for n in range(3, 6):
            put(at, acc_two[n], C2)
            at += C2
        put(at, acc_hid_two[...], HID2)
        at += HID2
        put(at, acc_two[6], C2)
        at += C2
        for n in range(7):
            put(at, acc_three[n], C3)
            at += C3
        put(at, acc_hid_three[...], HID3)
        at += HID3
        put(at, acc_three[7], C3)

    at_pair(pairs - 1, finish)


def run_main(places, place, buckets, state, goal, vec, weights, strip_count):
    pairs = goal.shape[0]
    slots = places[0].shape[0]
    half = slots // 2 + 1
    if pairs == 1:
        state = held_in(pltpu.VMEM, *state)
    weights = held_in(pltpu.VMEM, *weights)
    _, inv, _, mix, stat = state
    state_shapes = [STATE[1], STATE[3], STATE[4]]
    grad_kind = bf16 if pairs == 1 else f32
    wide_f32 = pltpu.VMEM((AREA, WIDE), f32)
    wide_bf16 = pltpu.VMEM((AREA, WIDE), bf16)
    scratch = [
        pltpu.VMEM((4, AREA + LINE, C2), f32),
        pltpu.VMEM((2, AREA, HID2), f32),
        pltpu.VMEM((4 * AREA, HID2), bf16),
        pltpu.VMEM((4 * AREA, HID2), bf16),
        pltpu.VMEM((4 * AREA, C2), bf16),
        pltpu.VMEM((4 * AREA, C2), bf16),
        pltpu.VMEM((AREA, 9 * C2), bf16),
        pltpu.VMEM((AREA + LINE, 9 * C2), f32),
        pltpu.VMEM((AREA, 128), f32),
        wide_f32,
        pltpu.VMEM((AREA + 2 * LINE, WIDE), f32),
        wide_f32,
        wide_f32,
        wide_f32,
        pltpu.VMEM((AREA, HID3), f32),
        pltpu.VMEM((AREA, HID3), f32),
        pltpu.VMEM((AREA, HID3), bf16),
        pltpu.VMEM((AREA, HID3), bf16),
        wide_bf16,
        wide_bf16,
        wide_bf16,
        pltpu.VMEM((C2, HID2), grad_kind),
        pltpu.VMEM((HID2, C2), grad_kind),
        pltpu.VMEM((9 * C2, WIDE), grad_kind),
        pltpu.VMEM((WIDE, HID3), grad_kind),
        pltpu.VMEM((HID3, WIDE), grad_kind),
        pltpu.VMEM((7, 8, C2), f32),
        pltpu.VMEM((8, HID2), f32),
        pltpu.VMEM((8, 8, WIDE), f32),
        pltpu.VMEM((8, HID3), f32),
    ]
    out_shapes = [(half, HALF, 128), (half, HALF, 128), (VEC_BLOCKS * HALF, 128)]
    make = pltpu.VMEM if pairs == 1 else jax.ShapeDtypeStruct
    return pl.pallas_call(
        functools.partial(main_kernel, pairs, strip_count, slots),
        grid=() if pairs == 1 else (pairs,),
        in_specs=[SMEM] * 4
        + pair_specs(pairs, state_shapes + [goal.shape[1:]], pl.Buffered(1))
        + whole_specs(pairs, [vec.shape])
        + [VMEM_BLOCK] * 5,
        out_specs=pair_specs(pairs, [(AREA, WIDE)] + BACK) + whole_specs(pairs, out_shapes),
        out_shape=pair_arrays(pairs, [(AREA, WIDE)] + BACK, [f32] * 4)
        + [make(shape, kind) for shape, kind in zip(out_shapes, (bf16, bf16, f32))],
        scratch_shapes=scratch,
        compiler_params=pltpu.CompilerParams(
            vmem_limit_bytes=(40 if pairs == 1 else 56) * 1024 * 1024,
            fuse_transposed_lhs_in_matmul=True,
        ),
        name="blocks",
    )(*places, place, buckets, inv, mix, stat, goal, vec, *weights)


def exit_kernel(
    pairs,
    strip_count,
    place_ref,
    bucket_ref,
    x_in,
    inv_in,
    pool_in,
    mix_in,
    stat_in,
    zed_in,
    dx_in,
    mean_in,
    flat_ref,
    vec_ref,
    payload_hbm,
    vector_ref,
    payload_ref,
    image_ref,
    col_ref,
    dx_ref,
    back_ref,
    acc_ref,
    sem,
):
    pair = pl.program_id(0) if pairs > 1 else 0
    x_ref, inv_ref, pool_ref, mix_ref, stat_ref, zed_ref, low_ref, mean_ref = (
        ref.at[0] for ref in (x_in, inv_in, pool_in, mix_in, stat_in, zed_in, dx_in, mean_in)
    )
    bucket_of = bucket_reader(place_ref, bucket_ref, strip_count)
    shape = Geometry(bucket_of, pair)
    count_two = shape.count_two
    gain1, bias1, scale1, gain2 = (vec_ref[n : n + 1] for n in range(4))
    mean1, scaling1, mean2, scaling2 = (stat_ref[n] for n in range(4))
    normal2 = (scaling2, -mean2 * scaling2)
    clear_edges(col_ref)
    nothing = jnp.zeros((8, C2), f32)
    back_gain2 = scaling2 * gain2
    back_mean2 = -scaling2 * mean_ref[0]
    back_normal2 = scaling2 * mean_ref[1]

    if pairs > 1:

        @pl.when(pair == 0)
        def _():
            acc_ref[...] = jnp.zeros(acc_ref.shape, f32)

    def add_up(n, total):
        acc_ref[n] = total if pairs == 1 else acc_ref[n] + total

    def unmix(k, d_scale):
        rows = step_rows(k)
        for pr in range(2):
            weighted = []
            for pc in range(2):
                plane = pr * 2 + pc
                share = inv_ref[plane, rows]
                normal = affine(mix_ref[plane, rows], *normal2)
                back = affine(low_ref[plane, rows], back_gain2, back_mean2)
                back = back - scaled(normal, back_normal2)
                d_mixed = jnp.where(share > 0.0, zed_ref[plane, rows] + back, 0.0)
                dx_ref[plane, rows] = d_mixed
                d_scale = d_scale + fold(pool_ref[plane, rows] * d_mixed)
                weighted.append(scale1 * d_mixed * share)
            put_col_windows(col_ref, pr, k, *weighted)
        return d_scale

    add_up(2, sweep(unmix, nothing))
    normal1 = (spread(scaling1, C2), spread(-mean1 * scaling1, C2))

    def unpool(k, carry):
        d_shift, d_gain = carry
        rows = step_rows(k)
        for pc in range(2):
            windows = row_windows(col_ref, pc, k)
            for pr in range(2):
                plane = pr * 2 + pc
                valid = inv_ref[plane, rows] > 0.0
                d_normal = windows[pr] - scale1 * dx_ref[plane, rows]
                d_normal = jnp.where(valid, d_normal, 0.0)
                back_ref[plane, rows] = d_normal
                normal = affine(x_ref[plane, rows], *normal1)
                d_shift = d_shift + fold(d_normal)
                d_gain = d_gain + fold(d_normal * normal)
        return (d_shift, d_gain)

    d_shift, d_gain = sweep(unpool, (nothing, nothing))
    add_up(1, d_shift)
    add_up(0, d_gain)
    mean_shift = by_image(d_shift * gain1) / count_two
    mean_gain = by_image(d_gain * gain1) / count_two
    back_gain1 = scaling1 * gain1
    back_mean1 = spread(-scaling1 * mean_shift, C2)
    back_normal1 = spread(scaling1 * mean_gain, C2)

    def unnorm(k, carry):
        rows = step_rows(k)
        for plane in range(4):
            normal = affine(x_ref[plane, rows], *normal1)
            back = affine(back_ref[plane, rows], back_gain1, back_mean1)
            back = back - scaled(normal, back_normal1)
            valid = inv_ref[plane, rows] > 0.0
            dx_ref[plane, rows] = jnp.where(valid, dx_ref[plane, rows] + back, 0.0)
        return carry

    sweep(unnorm, 0)

    def give_back(plane, here, spot, there):
        image_ref[spot, there] = dx_ref[plane, here]

    image_ref[...] = jnp.zeros(image_ref.shape, f32)
    each_image(bucket_of, pair, give_back)

    for spot in range(2 * STRIPS):
        target = strip_place(pair, spot, strip_count)
        for within in range(SR):
            rows = slice(within * CW, within * CW + CW)
            payload_ref[target, within] = image_ref[spot, rows].astype(bf16)

    def finish():
        copy = pltpu.make_async_copy(payload_ref, payload_hbm, sem)
        copy.start()
        vector_ref[...] = flat_ref[...]
        for n in range(3):
            vector_ref[n : n + 1] = jnp.sum(acc_ref[n], axis=0, keepdims=True)
        copy.wait()

    if pairs == 1:
        finish()
    else:
        pl.when(pair == pairs - 1)(finish)


def run_exit(place, buckets, state, back, flat, vec, strip_count):
    pairs = strip_count // 8
    payload = (strip_count, SR, CW, C2)
    make = pltpu.VMEM if pairs == 1 else jax.ShapeDtypeStruct
    plane_f32 = pltpu.VMEM((4, AREA, C2), f32)
    arrays = [*state, *back]
    if pairs == 1:
        arrays = held_in(pltpu.VMEM, *arrays)
    return pl.pallas_call(
        functools.partial(exit_kernel, pairs, strip_count),
        grid=() if pairs == 1 else (pairs,),
        in_specs=[SMEM] * 2
        + pair_specs(pairs, STATE + BACK, pl.Buffered(1))
        + whole_specs(pairs, [flat.shape, vec.shape]),
        out_specs=[HBM] + whole_specs(pairs, [flat.shape]),
        out_shape=[pltpu.HBM(payload, bf16), make(flat.shape, f32)],
        scratch_shapes=[
            pltpu.VMEM(payload, bf16),
            pltpu.VMEM((2 * STRIPS, STRIP_ROWS, C2), f32),
            pltpu.VMEM((4, AREA + 2 * LINE, C2), f32),
            plane_f32,
            plane_f32,
            pltpu.VMEM((3, 8, C2), f32),
            pltpu.SemaphoreType.DMA,
        ],
        compiler_params=roomy(8 if pairs == 1 else 40),
        name="exit",
    )(place, buckets, *arrays, flat, vec)


def dense_blocks(values):
    return jnp.concatenate([values[:, :HALF], values[:, HALF:]], axis=2).astype(bf16)


def pack_kernel(master_ref, dense_ref):
    dense_ref[...] = dense_blocks(master_ref[...])


def pack(master):
    owned = master.shape[0]
    return pl.pallas_call(
        pack_kernel,
        out_shape=jax.ShapeDtypeStruct((owned, HALF, 2 * BS), bf16),
        name="pack",
    )(master)


def pack_pieces_kernel(place_ref, master_hbm, pixel_hbm, *refs):
    out_refs, (wide_ref, master_ref, pixel_ref, sem) = refs[:-4], refs[-4:]
    owned = master_ref.shape[0]
    slots = pixel_ref.shape[2]
    copies = [pltpu.make_async_copy(pixel_hbm, pixel_ref, sem.at[0])]
    parts = [(0, owned // 2), (owned // 2, owned - owned // 2)]
    for n, part in enumerate(parts):
        copies.append(
            pltpu.make_async_copy(
                master_hbm.at[pl.ds(*part)], master_ref.at[pl.ds(*part)], sem.at[1 + n]
            )
        )
    for copy in copies:
        copy.start()
    copies[0].wait()

    def widen_row(row, carry):
        start = pl.multiple_of(row * CW * slots, 8)
        values = pixel_ref[row].astype(f32).reshape(CW * slots, C2)
        wide_ref[pl.ds(start, CW * slots)] = values
        return carry

    lax.fori_loop(0, SR, widen_row, 0)
    for k, ref in enumerate(out_refs):
        for other in range(2):
            slot = place_ref[0] ^ (2 * k + other)
            first = other * (ref.shape[0] - STRIP_ROWS)
            strip = wide_ref[pl.ds(slot, STRIP_ROWS, stride=slots)]
            ref[first : first + STRIP_ROWS] = strip.astype(bf16)
    for (first, count), copy in zip(parts, copies[1:]):
        copy.wait()
        dense = dense_blocks(master_ref[first : first + count]).reshape(count * HALF, 2 * BS)
        start = STRIP_ROWS + first * HALF
        for ref in out_refs[:3]:
            ref[start : start + count * HALF] = dense


def pack_pieces(place, master, pixels):
    slots = pixels.shape[2]
    rows = master.shape[0] * HALF
    shapes = [(rows + 2 * STRIP_ROWS, 2 * BS)] * 3 + [(2 * STRIP_ROWS, 2 * BS)]
    return pl.pallas_call(
        pack_pieces_kernel,
        in_specs=[SMEM] + [HBM] * 2,
        out_specs=[VMEM_BLOCK] * 4,
        out_shape=[pltpu.VMEM(shape, bf16) for shape in shapes],
        scratch_shapes=[
            pltpu.VMEM((STRIP_ROWS * slots, C2), f32),
            pltpu.VMEM(master.shape, f32),
            pltpu.VMEM(pixels.shape, bf16),
            pltpu.SemaphoreType.DMA((3,)),
        ],
        compiler_params=roomy(12),
        name="pack",
    )(place, *held_in(pltpu.HBM, master, pixels))


def fold_pair_kernel(near_ref, got_ref, own_ref, *part_refs):
    share = own_ref.shape[0]

    def one(n, carry):
        for k in range(len(part_refs) + 1):
            total = near_ref[k * share + n].astype(f32) + got_ref[k * share + n].astype(f32)
            if k == 0:
                own_ref[n] = total
            else:
                part_refs[k - 1][n] = total.astype(bf16)
        return carry

    lax.fori_loop(0, share, one, 0, unroll=4)


def fold_pair(near, got, groups):
    shape = ((near.shape[0] - 1) // groups,) + near.shape[1:]
    return pl.pallas_call(
        fold_pair_kernel,
        in_specs=[VMEM_BLOCK] * 2,
        out_specs=[VMEM_BLOCK] * groups,
        out_shape=[pltpu.VMEM(shape, f32)] + [pltpu.VMEM(shape, bf16)] * (groups - 1),
        compiler_params=roomy(4),
        name="fold_pair",
    )(*held_in(pltpu.VMEM, near, got))


def fold_tile_kernel(pieces, spot_ref, *refs):
    piece_refs, refs = refs[:pieces], refs[pieces:]
    vector_refs, refs = refs[:pieces], refs[pieces:]
    out_refs, sum_ref = refs[:-1], refs[-1]
    groups = len(out_refs)
    share = out_refs[0].shape[0]
    owned = piece_refs[0].shape[0]
    total = vector_refs[0][...]
    for ref in vector_refs[1:]:
        total = total + ref[...]
    for n in range(sum_ref.shape[0]):
        sum_ref[n] = jnp.zeros((HALF, 128), f32)
    for n in range(VEC_BLOCKS):
        sum_ref[n] = total[n * HALF : (n + 1) * HALF]

    def one(n, carry):
        for k, out_ref in enumerate(out_refs):
            number = lax.rem(spot_ref[0] + k, groups) * share + n
            block = jnp.minimum(number, owned - 1)
            total = piece_refs[0][block].astype(f32)
            for ref in piece_refs[1:]:
                total = total + ref[block].astype(f32)
            rest = sum_ref[jnp.maximum(number - owned, 0)]
            out_ref[n] = jnp.where(number < owned, total, rest).astype(out_ref.dtype)
        return carry

    lax.fori_loop(0, share, one, 0, unroll=share <= 16)


def fold_tile(spot, pieces, vectors, extra, groups):
    shape = ((pieces[0].shape[0] + extra) // groups,) + pieces[0].shape[1:]
    return pl.pallas_call(
        functools.partial(fold_tile_kernel, len(pieces)),
        in_specs=[SMEM] + [VMEM_BLOCK] * (len(pieces) + len(vectors)),
        out_specs=[VMEM_BLOCK] * groups,
        out_shape=[pltpu.VMEM(shape, f32)] + [pltpu.VMEM(shape, bf16)] * (groups - 1),
        scratch_shapes=[pltpu.VMEM((extra, HALF, 128), f32)],
        compiler_params=roomy(8),
        name="fold_tile",
    )(spot, *held_in(pltpu.VMEM, *pieces, *vectors))


def fold_batch_kernel(owned, vector_weight, spot_ref, *refs):
    part_refs, (total_ref, norm_ref) = refs[:-2], refs[-2:]
    share = total_ref.shape[0]
    square = jnp.zeros((8, 128), f32)
    for n in range(share):
        total = part_refs[0][n].astype(f32)
        for ref in part_refs[1:]:
            total = total + ref[n].astype(f32)
        total_ref[n] = total.astype(bf16)
        weight = jnp.where(spot_ref[0] * share + n < owned, 1.0, vector_weight)
        square = square + weight * fold(total * total)
    square = jnp.sum(jnp.sum(square, axis=1, keepdims=True), axis=0, keepdims=True)
    norm_ref[...] = jnp.broadcast_to(square[None], norm_ref.shape)


def fold_batch(spot, parts, owned, tile_count):
    count = tile_count * len(parts)
    return pl.pallas_call(
        functools.partial(fold_batch_kernel, owned, 1.0 / tile_count),
        in_specs=[SMEM] + [VMEM_BLOCK] * len(parts),
        out_specs=[VMEM_BLOCK] * 2,
        out_shape=[pltpu.VMEM(parts[0].shape, bf16), pltpu.VMEM((count, 1, 128), f32)],
        name="fold_batch",
    )(spot, *held_in(pltpu.VMEM, *parts))


def update_kernel(owned, groups, spot_ref, norm_ref, *refs):
    quarters, refs = refs[:groups], refs[groups:]
    stat_hbm, out_hbm, (vector_ref, clip_ref), refs = refs[:5], refs[5:10], refs[10:12], refs[12:]
    stat_refs, out_refs, (in_sem, out_sem) = refs[:5], refs[5:10], refs[10:]
    master_ref, left_stat_ref, right_stat_ref, left_root_ref, right_root_ref = stat_refs
    grad_ref, left_ref, right_ref, new_ref, copy_ref = out_refs
    share = quarters[0].shape[0]
    spans = spans_of(owned)

    def copies_of(sources, targets, sems):
        return [
            [
                pltpu.make_async_copy(
                    source.at[pl.ds(*span)], target.at[pl.ds(*span)], sems.at[5 * n + k]
                )
                for k, (source, target) in enumerate(zip(sources, targets))
            ]
            for n, span in enumerate(spans)
        ]

    copies_in = copies_of(stat_hbm, stat_refs, in_sem)
    copies_out = copies_of(out_refs, out_hbm, out_sem)
    for copies in copies_in:
        for copy in copies:
            copy.start()
    norm = jnp.sqrt(jnp.sum(norm_ref[...], axis=0))
    factor = jnp.minimum(1.0, clip_limit / norm)
    left_half = lax.broadcasted_iota(jnp.int32, (HALF, 128), 1) < BS

    def summed(number):
        source = number // share
        local = number - source * share
        turn = lax.rem(spot_ref[0] - source + groups, groups)
        value = quarters[0][local].astype(f32)
        for k in range(1, groups):
            value = jnp.where(turn == k, quarters[k][local].astype(f32), value)
        return value * factor

    def side_by_side(first, count):
        sides = []
        for n in range(first, first + count, 2):
            dense = summed(n)
            turned = pltpu.roll(dense, BS, 1)
            if n + 1 < first + count:
                second = summed(n + 1)
                top = jnp.where(left_half, dense, pltpu.roll(second, BS, 1))
                low = jnp.where(left_half, turned, second)
                side = jnp.concatenate([top, low], axis=0)
                grad_ref[n + 1] = pltpu.roll(side, BS, 1)[:, :BS]
            else:
                side = jnp.concatenate([dense, turned], axis=0)[:, :BS]
            grad_ref[n] = side[:, :BS]
            sides.append(side.astype(bf16))
        return jnp.concatenate(sides, axis=1)

    def diagonal_of(count):
        order = (count * BS, count * BS)
        return lax.broadcasted_iota(jnp.int32, order, 0) // BS == (
            lax.broadcasted_iota(jnp.int32, order, 1) // BS
        )

    clip_ref[...] = norm
    for n in range(vector_ref.shape[0]):
        vector_ref[n] = summed(owned + n)
    for (first, length), arriving, leaving in zip(spans, copies_in, copies_out):
        parts = [(n, min(4, first + length - n)) for n in range(first, first + length, 4)]
        wides = [side_by_side(*part) for part in parts]
        tall = [
            jnp.where(diagonal_of(count), jnp.concatenate([wide] * count, axis=0), 0.0)
            for (_, count), wide in zip(parts, wides)
        ]
        lefts = [product_nt(one, wide) for one, wide in zip(tall, wides)]
        rights = [product_tn(wide, wide) for wide in wides]
        for copy in arriving:
            copy.wait()
        stepped = []
        for (start, count), wide in zip(parts, wides):
            roots = left_root_ref[pl.ds(start, count)].reshape(count * BS, BS).astype(bf16)
            stepped.append(product(roots, wide))
        for (start, count), left, right in zip(parts, lefts, rights):
            here = pl.ds(start, count)
            left_ref[here] = 0.5 * left_stat_ref[here] + 0.5 * left.reshape(count, BS, BS)
            for n in range(count):
                at = n // 2 * 128
                block = right[n * BS : n * BS + BS, at : min(at + 128, count * BS)]
                if n % 2:
                    block = pltpu.roll(block, BS, 1)
                right_ref[start + n] = 0.5 * right_stat_ref[start + n] + 0.5 * block[:, :BS]
        for (start, count), value in zip(parts, stepped):
            here = pl.ds(start, count)
            value = jnp.where(diagonal_of(count), value, 0.0).astype(bf16)
            roots = right_root_ref[here].reshape(count * BS, BS).astype(bf16)
            value = product(value, roots).reshape(count, BS, BS)
            new = master_ref[here] - rate_matrix * value
            new_ref[here] = new
            copy_ref[here] = new.astype(bf16)
        for copy in leaving:
            copy.start()
    for leaving in copies_out:
        for copy in leaving:
            copy.wait()


def spans_of(owned):
    spans = []
    first = 0
    while first < owned:
        length = min(8 if first == 0 else 12, owned - first)
        spans.append((first, length))
        first += length
    return spans


def update(spot, norm, quarters, extra, *stats):
    shape = stats[0].shape
    groups = len(quarters)
    types = [f32] * 4 + [bf16]
    steps = len(spans_of(shape[0]))
    return pl.pallas_call(
        functools.partial(update_kernel, shape[0], groups),
        in_specs=[SMEM] + [VMEM_BLOCK] * (groups + 1) + [HBM] * 5,
        out_specs=[HBM] * 5 + [VMEM_BLOCK] * 2,
        out_shape=[pltpu.HBM(shape, kind) for kind in types]
        + [
            pltpu.VMEM((extra, HALF, 128), f32),
            pltpu.VMEM((1, 128), f32),
        ],
        scratch_shapes=[pltpu.VMEM(shape, f32)] * 5
        + [pltpu.VMEM(shape, kind) for kind in types]
        + [
            pltpu.SemaphoreType.DMA((5 * steps,)),
            pltpu.SemaphoreType.DMA((5 * steps,)),
        ],
        compiler_params=roomy(20),
        name="update",
    )(spot, *held_in(pltpu.VMEM, norm, *quarters), *held_in(pltpu.HBM, *stats))


def share_out(pieces, axis):
    return lax.all_to_all(pieces, axis, split_axis=0, concat_axis=0, tiled=True)


def swap(piece, distance):
    count = lax.axis_size("tile")
    return lax.ppermute(piece, "tile", [(i, i ^ distance) for i in range(count)])


def on_device(
    pixels,
    buckets,
    slot_owner_table,
    out_grad,
    master,
    left_stat,
    right_stat,
    left_root,
    right_root,
    vectors,
    moment,
):
    tile_count = lax.axis_size("tile")
    tile_place = lax.axis_index("tile")
    slot_count = pixels.shape[2]
    group_count = tile_count // STRIPS
    pairs = group_count // 2
    owned = master.shape[0]
    slots = owned * tile_count
    batch_count = lax.axis_size("batch")
    spot = lax.axis_index("batch").astype(jnp.int32).reshape(1)
    extra = extra_of(owned, batch_count)
    place = tile_place.astype(jnp.int32).reshape(1)
    paired = tile_count == 8
    numbers = jnp.arange(slots, dtype=jnp.int32)
    slot_of = jnp.sum(
        jnp.where(slot_owner_table[None, :] == numbers[:, None], numbers[None, :], 0), axis=1
    )
    if paired:
        owner = slot_of // owned
        apart = owner ^ tile_place
        apart = (apart & 1) * (tile_count // 2) + (apart >> 1)
        slot_of = slot_of + owned * (apart - owner)
    half = slots // 2
    near_place = jnp.where(slot_of < half, slot_of, half)
    far_place = jnp.where(slot_of < half, half, slot_of - half)
    vec = vectors.reshape(-1, 128)
    turned = lax.dynamic_index_in_dim(
        buckets.reshape(group_count, slot_count), tile_place, 1, keepdims=False
    ) >= 2
    flips = turned.reshape(-1, 1, 1, 1)
    goal = out_grad.reshape(2 * pairs, H3, W3, C3)
    goal = jnp.where(flips, goal.transpose(0, 2, 1, 3), goal)[:, :LINES]
    goal = goal.reshape(pairs, 2, LINES, W3, C3).transpose(0, 2, 3, 1, 4)
    goal = goal.reshape(pairs, LINES, 2 * W3, C3)
    goal = jnp.pad(goal, ((0, 0), (0, 0), (0, LINE - 2 * W3), (0, WIDE - C3)))
    goal = goal.reshape(pairs, AREA, WIDE)

    if paired:
        own, for_x, for_y, for_both = pack_pieces(
            place, master, pixels[0, 0].transpose(1, 2, 0, 3)
        )
        goal, vec, slot_of, near_place, far_place, own = lax.optimization_barrier(
            (goal, vec, slot_of, near_place, far_place, own)
        )
        from_x, from_y, strips_both = swap(for_x, 2), swap(for_y, 4), swap(for_both, 6)
        near_half = (owned + 1) // 2
        middle = STRIP_ROWS + near_half * HALF
        first_half = swap(from_x[STRIP_ROWS:middle], 4)
        second_half = swap(from_y[middle : STRIP_ROWS + owned * HALF], 2)
        mine = [own, from_x, from_y, strips_both, first_half, second_half]
        both = mine + [swap(piece, 1) for piece in mine]
        strips = both[:4] + both[6:10]
        pieces = [both[n] for n in (0, 1, 2, 4, 5, 6, 7, 8, 10, 11)]
        spans = [(STRIP_ROWS, owned)] * 3 + [(0, near_half), (0, owned - near_half)]
        spans = spans * 2
    else:
        pieces = [lax.all_gather(pack(master), "tile", axis=0, tiled=True).reshape(-1, 2 * BS)]
        spans = [(0, slots)]
        strips = share_out(pixels.reshape(tile_count, STRIP, C2), "tile")
        strips = [jnp.pad(strips, ((0, 0), (0, STRIP_ROWS - STRIP), (0, 0)))]

    weights = run_unpack(slot_of, pieces, spans)
    state = run_entry(place, buckets, strips, vec, tile_count)
    result, *back, near, far, flat = run_main(
        (near_place, far_place),
        place,
        buckets,
        state,
        goal,
        vec,
        weights,
        tile_count,
    )
    pixel_back, vector = run_exit(place, buckets, state, back, flat, vec, tile_count)
    if paired:
        own, *parts = fold_pair(near, swap(far, 1), tile_count // 2)
        pieces = [own] + [swap(part, 2 * k + 2) for k, part in enumerate(parts)]
        vector, _ = lax.optimization_barrier((vector, parts[0]))
        vector = vector + swap(vector, 1)
        vectors_in = [vector] + [swap(vector, 2 * k) for k in range(1, tile_count // 2)]
    else:
        outgoing = jnp.concatenate([near[:half], far[:half]], axis=0)
        pieces = list(share_out(outgoing.reshape(tile_count, owned, HALF, 128), "tile"))
        vectors_in = list(lax.all_gather(vector, "tile"))
    result, pieces[1] = lax.optimization_barrier((result, pieces[1]))
    result = result.reshape(pairs, LINES, LINE, WIDE)[:, :, : 2 * W3, :C3]
    result = result.reshape(pairs, LINES, W3, 2, C3).transpose(0, 3, 1, 2, 4)
    result = result.reshape(2 * pairs, LINES, W3, C3)
    result = jnp.pad(result, ((0, 0), (0, H3 - LINES), (0, 0), (0, 0)))
    result = jnp.where(flips, result.transpose(0, 2, 1, 3), result)
    result = result.reshape(out_grad.shape)
    result = with_layout_constraint(result, Layout(major_to_minor=(0, 1, 2, 4, 5, 3, 6)))
    result, vectors_in[0] = lax.optimization_barrier((result, vectors_in[0]))
    own, *parts = fold_tile(spot, pieces, vectors_in, extra, batch_count)
    pixel_back, parts[0] = lax.optimization_barrier((pixel_back, parts[0]))
    returned = share_out(pixel_back, "tile")
    parts = [
        lax.ppermute(part, "batch", [(i, (i + k + 1) % batch_count) for i in range(batch_count)])
        for k, part in enumerate(parts)
    ]
    quarter, norm = fold_batch(spot, [own] + parts, owned, tile_count)
    returned, norm = lax.optimization_barrier((returned, norm))
    norm = share_out(norm, ("batch", "tile"))
    returned = returned.astype(f32).reshape(pixels.shape)
    returned = with_layout_constraint(returned, Layout(major_to_minor=(0, 1, 3, 4, 2, 5)))
    returned, quarter = lax.optimization_barrier((returned, quarter))
    quarters = [quarter] + [
        lax.ppermute(quarter, "batch", [(i, (i + k) % batch_count) for i in range(batch_count)])
        for k in range(1, batch_count)
    ]
    block_grad, left_new, right_new, master_new, weight_copy, whole_vector, clip = update(
        spot, norm, quarters, extra, master, left_stat, right_stat, left_root, right_root
    )
    clip_norm = clip[0, 0]
    share = vectors.shape[0] // tile_count
    whole_vector = whole_vector.reshape(-1)
    vec_grad = lax.dynamic_slice_in_dim(whole_vector, tile_place * share, share, 0)
    vec_moment = moment + vec_grad * vec_grad
    own_vectors = lax.dynamic_slice_in_dim(vectors, tile_place * share, share, 0)
    vec_new = own_vectors - rate_vector * vec_grad / (jnp.sqrt(vec_moment) + eps_adagrad)
    return (
        result,
        returned,
        clip_norm,
        block_grad,
        left_new,
        right_new,
        master_new,
        weight_copy,
        vec_grad,
        vec_moment,
        vec_new,
    )


def solution(mesh):
    placed = (
        P("batch", "tile", None, None, None, None),
        P("batch"),
        P(),
        P("batch", "tile", None, None, None, None, None),
        P("tile", None, None),
        P("tile", None, None),
        P("tile", None, None),
        P("tile", None, None),
        P("tile", None, None),
        P(),
        P("tile"),
    )
    return jax.shard_map(
        on_device,
        mesh=mesh,
        in_specs=placed,
        out_specs=(
            P("batch", "tile", None, None, None, None, None),
            P("batch", "tile", None, None, None, None),
            P(),
            P("tile", None, None),
            P("tile", None, None),
            P("tile", None, None),
            P("tile", None, None),
            P("tile", None, None),
            P("tile"),
            P("tile"),
            P("tile"),
        ),
        check_vma=False,
    )
```

```python
import functools

import jax
import jax.numpy as jnp
from jax import lax
from jax.experimental import pallas as pl
from jax.experimental.layout import Layout, with_layout_constraint
from jax.experimental.pallas import tpu as pltpu
from jax.sharding import PartitionSpec as P

C2 = 128
HID2 = 512
C3 = 320
HID3 = 1280
CH = 36
CW = 36
STRIPS = 4
BS = 64
SR = CH // STRIPS
H3 = CH // 2
W3 = CW // 2
LONG = 7 * CH // 9
LINES = LONG // 2
WIDE = 384
LINE = 40
AREA = LINES * LINE
STEP = 2 * LINE
STEPS = AREA // STEP
HALF = BS // 2
STRIP = SR * CW
STRIP_ROWS = STRIP + -STRIP % 16

eps_norm = 1e-05
clip_limit = 1.0
rate_matrix = 0.3
rate_vector = 0.3
eps_adagrad = 1e-08
f32 = jnp.float32
bf16 = jnp.bfloat16

SHAPES = [(C2, HID2), (HID2, C2), (9 * C2, C3), (C3, HID3), (HID3, C3)]
USED = sum(rows // BS * (cols // BS) for rows, cols in SHAPES)
VEC_ROWS = (6 * C2 + HID2 + C2 + C3 + 6 * C3 + HID3 + C3) // 128


VEC_BLOCKS = -(-VEC_ROWS // HALF)


def extra_of(owned, groups):
    return VEC_BLOCKS + -(owned + VEC_BLOCKS) % groups


def product(left, right):
    return jnp.dot(left, right, preferred_element_type=f32)


def product_nt(left, right):
    return lax.dot_general(left, right, (((1,), (1,)), ((), ())), preferred_element_type=f32)


def product_tn(left, right):
    return lax.dot_general(left, right, (((0,), (0,)), ((), ())), preferred_element_type=f32)


def gelu_pair(values):
    bell = jnp.exp2(values * values * (-0.5 * 1.4426950408889634))
    step = pl.reciprocal(1.0 + (0.3275911 * 0.7071067811865476) * jnp.abs(values), approx=True)
    tail = step * (
        0.5 * 0.254829592
        + step
        * (
            0.5 * -0.284496736
            + step
            * (0.5 * 1.421413741 + step * (0.5 * -1.453152027 + step * (0.5 * 1.061405429)))
        )
    )
    tail = tail * bell
    share = jnp.where(values >= 0.0, 1.0 - tail, tail)
    return (values * share, share + values * (bell * 0.3989422804014327))


def fold(values):
    chans = values.shape[-1]
    return jnp.sum(values.reshape(-1, 8, chans), axis=0)


def by_image(total):
    total = total + pltpu.roll(total, 4, 0)
    total = total + pltpu.roll(total, 2, 0)
    return jnp.sum(total, axis=1, keepdims=True)


def line(pattern):
    return jnp.concatenate([pattern] * (LINE // 8), axis=0)


def spread(pattern, chans):
    return jnp.broadcast_to(pattern, (8, chans))


def affine(values, factor, shift):
    tiles = values.reshape(-1, 8, values.shape[-1])
    return (tiles * factor + shift).reshape(values.shape)


def scaled(values, factor):
    tiles = values.reshape(-1, 8, values.shape[-1])
    return (tiles * factor).reshape(values.shape)


def from_left(values):
    return pltpu.roll(values, 2, 0)


def from_right(values):
    return pltpu.roll(values, values.shape[0] - 2, 0)


def rounded(values):
    return values.astype(bf16).astype(f32)


def widen(values):
    return jnp.concatenate([values] * (WIDE // 128), axis=-1)


def norm_terms(total, square, count):
    mean = by_image(total) / count
    scaling = lax.rsqrt(by_image(square) / count - mean * mean + eps_norm)
    return (mean, scaling)


def sweep(visit, start):
    return lax.fori_loop(0, STEPS, visit, start, unroll=True)


def step_rows(k, lines=0):
    start = k * STEP + lines * LINE
    return pl.ds(start if isinstance(k, int) else pl.multiple_of(start, LINE), STEP)


def held_in(space, *arrays):
    return [pltpu.with_memory_space_constraint(array, space) for array in arrays]


VMEM_BLOCK = pl.BlockSpec(memory_space=pltpu.VMEM)
HBM = pl.BlockSpec(memory_space=pltpu.HBM)
SMEM = pl.BlockSpec(memory_space=pltpu.SMEM)


def roomy(mebibytes):
    return pltpu.CompilerParams(vmem_limit_bytes=mebibytes * 1024 * 1024)


def image_shape(bucket_of, pair, image):
    bucket = bucket_of(2 * pair + image)
    plain = jnp.where(bucket == 0, 5 * CH // 9, 7 * CH // 9)
    across = jnp.where(bucket == 0, CW, 7 * CW // 9)
    turned = (bucket >= 2).astype(jnp.int32)
    return (
        jnp.where(turned > 0, 5 * CW // 9, plain),
        jnp.where(turned > 0, CH, across),
        turned,
    )


def bucket_reader(place_ref, bucket_ref, strip_count):
    return lambda group: bucket_ref[group * strip_count + place_ref[0]]


class Geometry:
    def __init__(self, bucket_of, pair):
        parity = lax.broadcasted_iota(jnp.int32, (8, 128), 0) % 2
        even, odd = (image_shape(bucket_of, pair, image) for image in range(2))
        high, broad, turned = (jnp.where(parity == 0, a, b) for a, b in zip(even, odd))
        self.high = high
        self.count_two = (high * broad * C2).astype(f32)[:, :1]
        self.high3 = (high + 1) // 2
        broad3 = (broad + 1) // 2
        self.count_three = (self.high3 * broad3 * C3).astype(f32)[:, :1]
        place = lax.broadcasted_iota(jnp.int32, (LINE, 128), 0) // 2
        inside = lax.broadcasted_iota(jnp.int32, (LINE, 128), 0) < 2 * W3
        self.reach = []
        self.col_share = []
        for pc in range(2):
            column = 2 * place + pc
            self.reach.append(jnp.where(inside & (column < line(broad)), line(high), 0))
            edge = (column == 0) | (column == line(broad) - 1)
            self.col_share.append(jnp.where(edge, 0.5, 1.0 / 3.0))
        self.reach3 = jnp.where(inside & (place < line(broad3)), line(self.high3), 0)
        edge3 = (place == 0) | (place == line(broad3) - 1)
        self.col_share3 = jnp.where(edge3, 0.5, 1.0 / 3.0)
        self.flipped = jnp.concatenate([turned] * (STEP // 8), axis=0) > 0

    def share(self, plane, k):
        pr, pc = plane // 2, plane % 2
        return self.lines(4 * k + pr, 2, self.reach[pc], self.col_share[pc], self.high)

    def share3(self, k):
        return self.lines(2 * k, 1, self.reach3, self.col_share3, self.high3)

    def lines(self, row, stride, reach, col_share, height):
        parts = []
        for n in range(2):
            here = row + stride * n
            row_share = jnp.where((here == 0) | (here == height - 1), 0.5, 1.0 / 3.0)
            parts.append(jnp.where(here < reach, line(row_share) * col_share, 0.0))
        return jnp.concatenate(parts, axis=0)


def strip_place(pair, spot, strip_count):
    return lax.rem(pair * 8 + strip_count - 2 + spot, strip_count)


def each_image(bucket_of, pair, visit):
    for image in range(2):
        way = image_shape(bucket_of, pair, image)[2]

        @pl.when(way == 0)
        def _():
            def one(r, carry):
                for plane in range(4):
                    row = 2 * r + plane // 2
                    strip = row // SR
                    there = pl.ds((row - strip * SR) * CW + plane % 2, W3, stride=2)
                    here = pl.ds(r * LINE + image, W3, stride=2)
                    visit(plane, here, image * STRIPS + strip, there)
                return carry

            lax.fori_loop(0, LINES, one, 0)

        @pl.when(way == 1)
        def _():
            def one(r, carry):
                for plane in range(4):
                    for strip in range(STRIPS):
                        first = (plane % 2 + strip * SR) % 2
                        count = (SR - first + 1) // 2
                        done = (strip * SR + first) // 2
                        column = 2 * r + plane // 2
                        there = pl.ds(first * CW + column, count, stride=2 * CW)
                        here = pl.ds(r * LINE + image + 2 * done, count, stride=2)
                        visit(plane, here, image * STRIPS + strip, there)
                return carry

            lax.fori_loop(0, LINES, one, 0)


def row_windows(col_ref, pc, k):
    both = col_ref[pc, step_rows(k, 1)] + col_ref[2 + pc, step_rows(k, 1)]
    return (both + col_ref[2 + pc, step_rows(k)], both + col_ref[pc, step_rows(k, 2)])


def put_col_windows(col_ref, pr, k, even, odd):
    both = even + odd
    col_ref[pr * 2, step_rows(k, 1)] = both + from_left(odd)
    col_ref[pr * 2 + 1, step_rows(k, 1)] = both + from_right(even)


def clear_edges(col_ref):
    zero_line = jnp.zeros((LINE, C2), f32)
    for plane in range(4):
        col_ref[plane, 0:LINE] = zero_line
        col_ref[plane, AREA + LINE : AREA + 2 * LINE] = zero_line


def entry_kernel(pairs, strip_count, piece_count, place_ref, bucket_ref, vec_ref, *refs):
    piece_refs, refs = refs[:piece_count], refs[piece_count:]
    x_out, inv_out, pool_out, mix_out, stat_out, image_ref, col_ref = refs
    pair = pl.program_id(0) if pairs > 1 else 0
    x_ref, inv_ref, pool_ref, mix_ref = (ref.at[0] for ref in (x_out, inv_out, pool_out, mix_out))
    bucket_of = bucket_reader(place_ref, bucket_ref, strip_count)
    shape = Geometry(bucket_of, pair)
    gain1, bias1, scale1 = (vec_ref[n : n + 1] for n in range(3))
    clear_edges(col_ref)
    if piece_count > 1:
        half = piece_count // 2
        for n, ref in enumerate(piece_refs):
            source = place_ref[0] ^ (n // half + 2 * (n % half))
            spot = lax.rem(source + 2, 2 * STRIPS)
            first = 0 if n < half else ref.shape[0] - STRIP_ROWS
            image_ref[spot] = ref[first : first + STRIP_ROWS].astype(f32)
    else:
        for spot in range(2 * STRIPS):
            source = strip_place(pair, spot, strip_count)
            image_ref[spot] = piece_refs[0][source].astype(f32)

    def take_in(plane, here, spot, there):
        x_ref[plane, here] = image_ref[spot, there]

    each_image(bucket_of, pair, take_in)

    def arrange(k, carry):
        total, square = carry
        rows = step_rows(k)
        for plane in range(4):
            share = shape.share(plane, k)
            inv_ref[plane, rows] = share
            values = jnp.where(share > 0.0, x_ref[plane, rows], 0.0)
            x_ref[plane, rows] = values
            total = total + fold(values)
            square = square + fold(values * values)
        return (total, square)

    nothing = jnp.zeros((8, C2), f32)
    total, square = sweep(arrange, (nothing, nothing))
    mean1, scaling1 = norm_terms(total, square, shape.count_two)
    factor1 = scaling1 * gain1
    shift1 = bias1 - mean1 * scaling1 * gain1

    def window_cols(k, carry):
        rows = step_rows(k)
        for pr in range(2):
            masked = []
            for pc in range(2):
                plane = pr * 2 + pc
                normal = rounded(affine(x_ref[plane, rows], factor1, shift1))
                masked.append(jnp.where(inv_ref[plane, rows] > 0.0, normal, 0.0))
            put_col_windows(col_ref, pr, k, *masked)
        return carry

    sweep(window_cols, 0)

    def mix(k, carry):
        total, square = carry
        rows = step_rows(k)
        for pc in range(2):
            windows = row_windows(col_ref, pc, k)
            for pr in range(2):
                plane = pr * 2 + pc
                values = x_ref[plane, rows]
                share = inv_ref[plane, rows]
                pooled = windows[pr] * share - rounded(affine(values, factor1, shift1))
                pooled = jnp.where(share > 0.0, pooled, 0.0)
                mixed = values + scale1 * pooled
                pool_ref[plane, rows] = pooled
                mix_ref[plane, rows] = mixed
                total = total + fold(mixed)
                square = square + fold(mixed * mixed)
        return (total, square)

    total, square = sweep(mix, (nothing, nothing))
    mean2, scaling2 = norm_terms(total, square, shape.count_two)
    for n, value in enumerate((mean1, scaling1, mean2, scaling2)):
        stat_out[0, n] = spread(value, 128)


def pair_specs(pairs, shapes, mode=None):
    if pairs == 1:
        return [VMEM_BLOCK] * len(shapes)
    return [
        pl.BlockSpec(
            (1,) + shape, lambda t, rank=len(shape): (t,) + (0,) * rank, pipeline_mode=mode
        )
        for shape in shapes
    ]


def whole_specs(pairs, shapes):
    if pairs == 1:
        return [VMEM_BLOCK] * len(shapes)
    return [
        pl.BlockSpec(
            shape,
            lambda t, rank=len(shape): (0,) * rank,
            pipeline_mode=pl.Buffered(1),
        )
        for shape in shapes
    ]


def pair_arrays(pairs, shapes, kinds):
    make = pltpu.VMEM if pairs == 1 else jax.ShapeDtypeStruct
    return [make((pairs,) + shape, kind) for shape, kind in zip(shapes, kinds)]


STATE = [(4, AREA, C2)] * 4 + [(4, 8, 128)]
BACK = [(4, AREA, C2)] * 2 + [(2, 8, 128)]


def run_entry(place, buckets, pieces, vec, strip_count):
    pairs = strip_count // 8
    if pairs == 1:
        pieces = held_in(pltpu.VMEM, *pieces)
    return pl.pallas_call(
        functools.partial(entry_kernel, pairs, strip_count, len(pieces)),
        grid=() if pairs == 1 else (pairs,),
        in_specs=[SMEM] * 2 + whole_specs(pairs, [array.shape for array in (vec, *pieces)]),
        out_specs=pair_specs(pairs, STATE),
        out_shape=pair_arrays(pairs, STATE, [f32] * 5),
        scratch_shapes=[
            pltpu.VMEM((2 * STRIPS, STRIP_ROWS, C2), f32),
            pltpu.VMEM((4, AREA + 2 * LINE, C2), f32),
        ],
        compiler_params=roomy(6 if pairs == 1 else 40),
        name="entry",
    )(place, buckets, vec, *pieces)


WEIGHTS = [(C2, HID2), (HID2, C2), (9 * C2, WIDE), (WIDE, HID3), (HID3, WIDE)]


def unpack_kernel(spans, slot_ref, *refs):
    piece_refs, refs = refs[: len(spans)], refs[len(spans) :]
    weights, gathered_ref = refs[:-1], refs[-1]
    done = 0
    for ref, (first, count) in zip(piece_refs, spans):
        blocks = ref[first : first + count * HALF].reshape(count, HALF, 128)
        gathered_ref[done : done + count] = blocks
        done += count
    left_half = lax.broadcasted_iota(jnp.int32, (HALF, 128), 1) < BS
    offset = 0
    for (rows, cols), ref in zip(SHAPES, weights):
        wide = cols // BS
        for rb in range(rows // BS):
            for cb in range(0, wide, 2):
                number = offset + rb * wide + cb
                first = gathered_ref[slot_ref[number]]
                turned = pltpu.roll(first, BS, 1)
                if cb + 1 < wide:
                    second = gathered_ref[slot_ref[number + 1]]
                    top = jnp.where(left_half, first, pltpu.roll(second, BS, 1))
                    low = jnp.where(left_half, turned, second)
                else:
                    top = jnp.where(left_half, first, 0.0)
                    low = jnp.where(left_half, turned, 0.0)
                place = slice(cb * BS, cb * BS + 128)
                ref[rb * BS : rb * BS + HALF, place] = top
                ref[rb * BS + HALF : rb * BS + BS, place] = low
        offset += rows // BS * wide
    weights[3][C3:, :] = jnp.zeros((WIDE - C3, HID3), bf16)


def run_unpack(slot_of, pieces, spans):
    slots = slot_of.shape[0]
    return pl.pallas_call(
        functools.partial(unpack_kernel, spans),
        in_specs=[SMEM] + [VMEM_BLOCK] * len(pieces),
        out_specs=[VMEM_BLOCK] * 5,
        out_shape=[pltpu.VMEM(shape, bf16) for shape in WEIGHTS],
        scratch_shapes=[pltpu.VMEM((slots, HALF, 128), bf16)],
        compiler_params=roomy(6),
        name="unpack",
    )(slot_of, *held_in(pltpu.VMEM, *pieces))


def main_kernel(
    pairs,
    strip_count,
    slots,
    near_place,
    far_place,
    place_ref,
    bucket_ref,
    inv_in,
    mix_in,
    stat_in,
    goal_ref,
    vec_ref,
    w1_ref,
    w2_ref,
    we_ref,
    w3_ref,
    w4_ref,
    result_ref,
    zed_out,
    dx_out,
    mean_out,
    near_ref,
    far_ref,
    flat_ref,
    zed_ref,
    hid_ref,
    u_ref,
    g_ref,
    h_ref,
    dy_ref,
    patch_ref,
    dpatch_ref,
    inv3_ref,
    e_ref,
    col3_ref,
    pool3_ref,
    mix3_ref,
    dx3_ref,
    hid3_ref,
    dhid3_ref,
    u3_ref,
    g3_ref,
    h3_ref,
    dy3_ref,
    dpre_ref,
    gw1_ref,
    gw2_ref,
    gwe_ref,
    gw3_ref,
    gw4_ref,
    acc_two,
    acc_hid_two,
    acc_three,
    acc_hid_three,
):
    pair = pl.program_id(0) if pairs > 1 else 0
    grads = [gw1_ref, gw2_ref, gwe_ref, gw3_ref, gw4_ref]
    inv_ref, mix_ref, stat_ref = (ref.at[0] for ref in (inv_in, mix_in, stat_in))
    back_ref, dx_ref = zed_out.at[0], dx_out.at[0]
    left_half = lax.broadcasted_iota(jnp.int32, (HALF, 128), 1) < BS

    def at_pair(number, act):
        if pairs == 1:
            act()
        else:
            pl.when(pair == number)(act)

    def begin():
        acc_two[...] = jnp.zeros(acc_two.shape, f32)
        acc_hid_two[...] = jnp.zeros(acc_hid_two.shape, f32)
        acc_three[...] = jnp.zeros(acc_three.shape, f32)
        acc_hid_three[...] = jnp.zeros(acc_hid_three.shape, f32)

    at_pair(0, begin)
    shape = Geometry(bucket_reader(place_ref, bucket_ref, strip_count), pair)
    count_two, count_three, flipped = shape.count_two, shape.count_three, shape.flipped
    nothing = jnp.zeros((8, C2), f32)
    nothing3 = jnp.zeros((8, WIDE), f32)

    def vector_row(at, length):
        first, shift = at // 128, at % 128
        count = -(-(shift + length) // 128)
        row = jnp.concatenate([vec_ref[first + n : first + n + 1] for n in range(count)], axis=1)
        if shift:
            row = pltpu.roll(jnp.broadcast_to(row, (8, count * 128)), count * 128 - shift, 1)[:1]
        return row

    def wide_row(at):
        lane = lax.broadcasted_iota(jnp.int32, (1, WIDE), 1)
        return jnp.where(lane < C3, vector_row(at, C3)[:, :WIDE], 0.0)

    gain2, bias2, scale2 = (vec_ref[n : n + 1] for n in range(3, 6))
    hid_bias = vector_row(6 * C2, HID2)
    out_bias = vector_row(6 * C2 + HID2, C2)
    two = 7 * C2 + HID2
    embed_bias, gain3, bias3, scale3 = (wide_row(two + n * C3) for n in range(4))
    gain4, bias4, scale4 = (wide_row(two + n * C3) for n in range(4, 7))
    hid_bias3 = vector_row(two + 7 * C3, HID3)[:, :HID3]
    out_bias3 = wide_row(two + 7 * C3 + HID3)
    mean2, scaling2 = stat_ref[2], stat_ref[3]
    factor2 = scaling2 * gain2
    shift2 = bias2 - mean2 * scaling2 * gain2
    for plane in range(4):
        zed_ref[plane, 0:LINE] = jnp.zeros((LINE, C2), f32)
    col3_ref[0:LINE] = jnp.zeros((LINE, WIDE), f32)
    col3_ref[AREA + LINE : AREA + 2 * LINE] = jnp.zeros((LINE, WIDE), f32)

    def put_block(number, block):
        near_ref[near_place[number]] = block
        far_ref[far_place[number]] = block

    def pack_blocks(matrices):
        offsets = [0]
        for rows, cols in SHAPES:
            offsets.append(offsets[-1] + rows // BS * (cols // BS))
        for which in matrices:
            (rows, cols), ref = SHAPES[which], grads[which]
            wide = cols // BS
            for rb in range(rows // BS):
                for cb in range(0, wide, 2):
                    number = offsets[which] + rb * wide + cb
                    at = slice(cb * BS, cb * BS + 128)
                    top = ref[rb * BS : rb * BS + HALF, at].astype(bf16)
                    low = ref[rb * BS + HALF : rb * BS + BS, at].astype(bf16)
                    put_block(number, jnp.where(left_half, top, pltpu.roll(low, BS, 1)))
                    if cb + 1 < wide:
                        put_block(number + 1, jnp.where(left_half, pltpu.roll(top, BS, 1), low))

    def plane_rows(plane):
        return slice(plane * AREA, plane * AREA + AREA)

    def begin_plane(plane):
        low = affine(mix_ref[plane], factor2, shift2).astype(bf16)
        h_ref[plane_rows(plane)] = low
        hid_ref[plane % 2] = product(low, w1_ref[...])

    begin_plane(0)
    for plane in range(4):
        if plane < 3:
            begin_plane(plane + 1)
        for k in range(STEPS):
            rows = step_rows(k)
            flat = slice(plane * AREA + k * STEP, plane * AREA + k * STEP + STEP)
            for at in range(0, HID2, 128):
                lanes = slice(at, at + 128)
                active, slope = gelu_pair(hid_ref[plane % 2, rows, lanes] + hid_bias[:, lanes])
                u_ref[flat, lanes] = active.astype(bf16)
                g_ref[flat, lanes] = slope.astype(bf16)
        out = product(u_ref[plane_rows(plane)], w2_ref[...]) + out_bias
        zed = jnp.where(inv_ref[plane] > 0.0, mix_ref[plane] + scale2 * out, 0.0)
        zed_ref[plane, LINE : LINE + AREA] = rounded(zed)

    def patches(k, carry):
        rows = step_rows(k)
        taps = []
        for ky in range(3):
            pr = (0 if ky == 1 else 1) * 2
            source = step_rows(k, 0 if ky == 0 else 1)
            even = zed_ref[pr, source]
            odd = zed_ref[pr + 1, source]
            taps.append((from_left(odd), even, odd))
        for ky in range(3):
            for kx in range(3):
                at = (3 * ky + kx) * C2
                tap = taps[ky][kx]
                if ky != kx:
                    tap = jnp.where(flipped, taps[kx][ky], tap)
                patch_ref[rows, at : at + C2] = tap.astype(bf16)
        return carry

    sweep(patches, 0)
    e_ref[...] = product(patch_ref[...], we_ref[...])

    def embed(k, carry):
        total, square = carry
        rows = step_rows(k)
        share = shape.share3(k)
        inv3_ref[rows] = share
        out = jnp.where(widen(share) > 0.0, e_ref[rows] + embed_bias, 0.0)
        e_ref[rows] = out
        return (total + fold(out), square + fold(out * out))

    total, square = sweep(embed, (nothing3, nothing3))
    mean3, scaling3 = norm_terms(total, square, count_three)
    factor3 = scaling3 * gain3
    shift3 = bias3 - mean3 * scaling3 * gain3

    def window_cols3(k, carry):
        rows = step_rows(k)
        normal = rounded(affine(e_ref[rows], factor3, shift3))
        masked = jnp.where(widen(inv3_ref[rows]) > 0.0, normal, 0.0)
        col3_ref[step_rows(k, 1)] = masked + from_left(masked) + from_right(masked)
        return carry

    sweep(window_cols3, 0)

    def row_windows3(k):
        return col3_ref[step_rows(k)] + col3_ref[step_rows(k, 1)] + col3_ref[step_rows(k, 2)]

    def mix3(k, carry):
        total, square = carry
        rows = step_rows(k)
        values = e_ref[rows]
        share = widen(inv3_ref[rows])
        pooled = row_windows3(k) * share - rounded(affine(values, factor3, shift3))
        pooled = jnp.where(share > 0.0, pooled, 0.0)
        mixed = values + scale3 * pooled
        pool3_ref[rows] = pooled
        mix3_ref[rows] = mixed
        return (total + fold(mixed), square + fold(mixed * mixed))

    total, square = sweep(mix3, (nothing3, nothing3))
    mean4, scaling4 = norm_terms(total, square, count_three)
    factor4 = scaling4 * gain4
    shift4 = bias4 - mean4 * scaling4 * gain4
    normal4 = (spread(scaling4, WIDE), spread(-mean4 * scaling4, WIDE))

    def prepare3(k, d_bias):
        rows = step_rows(k)
        h3_ref[rows] = affine(mix3_ref[rows], factor4, shift4).astype(bf16)
        goal = goal_ref[0, rows].astype(f32)
        goal = jnp.where(widen(inv3_ref[rows]) > 0.0, goal, 0.0)
        low_goal = (scale4 * goal).astype(bf16)
        dy3_ref[rows] = low_goal
        return d_bias + fold(low_goal.astype(f32))

    acc_three[7] += sweep(prepare3, nothing3)

    def keep(ref, value, place=slice(None)):
        if pairs == 1:
            ref[place] = value.astype(ref.dtype)
        else:

            @pl.when(pair == 0)
            def _():
                ref[place] = value

            @pl.when(pair > 0)
            def _():
                ref[place] += value

    def begin_chunk(at):
        lanes = slice(at, at + 256)
        hid3_ref[:, lanes] = product(h3_ref[...], w3_ref[:, lanes])
        dhid3_ref[:, lanes] = product_nt(dy3_ref[...], w4_ref[lanes])

    begin_chunk(0)
    for at in range(0, HID3, 256):
        if at + 256 < HID3:
            begin_chunk(at + 256)
        for lane in (at, at + 128):
            lanes = slice(lane, lane + 128)
            total = nothing
            for k in range(STEPS):
                rows = step_rows(k)
                active, slope = gelu_pair(hid3_ref[rows, lanes] + hid_bias3[:, lanes])
                u3_ref[rows, lanes] = active.astype(bf16)
                low = (slope * dhid3_ref[rows, lanes]).astype(bf16)
                g3_ref[rows, lanes] = low
                total = total + fold(low.astype(f32))
            acc_hid_three[:, lanes] += total
        lanes = slice(at, at + 256)
        out = product(u3_ref[:, lanes], w4_ref[lanes])
        d_low = product_nt(g3_ref[:, lanes], w3_ref[:, lanes])
        result_ref[0] = out if at == 0 else result_ref[0] + out
        dx3_ref[...] = d_low if at == 0 else dx3_ref[...] + d_low
        keep(gw3_ref, product_tn(h3_ref[...], g3_ref[:, lanes]), (slice(None), lanes))
        keep(gw4_ref, product_tn(u3_ref[:, lanes], dy3_ref[...]), lanes)

    def finish3(k, carry):
        d_scale, d_shift, d_gain = carry
        rows = step_rows(k)
        valid = widen(inv3_ref[rows]) > 0.0
        mixed = mix3_ref[rows]
        out = jnp.where(valid, result_ref[0, rows] + out_bias3, 0.0)
        result_ref[0, rows] = mixed + scale4 * out
        d_scale = d_scale + fold(out * goal_ref[0, rows].astype(f32))
        d_low = dx3_ref[rows]
        normal = affine(mixed, *normal4)
        return (d_scale, d_shift + fold(d_low), d_gain + fold(d_low * normal))

    d_scale, d_shift, d_gain = sweep(finish3, (nothing3, nothing3, nothing3))
    acc_three[6] += d_scale
    acc_three[5] += d_shift
    acc_three[4] += d_gain
    mean_shift = by_image(d_shift * gain4) / count_three
    mean_gain = by_image(d_gain * gain4) / count_three
    back_gain4 = scaling4 * gain4
    back_mean4 = spread(-scaling4 * mean_shift, WIDE)
    back_normal4 = spread(scaling4 * mean_gain, WIDE)

    def unmix3(k, d_scale):
        rows = step_rows(k)
        share = widen(inv3_ref[rows])
        valid = share > 0.0
        normal = affine(mix3_ref[rows], *normal4)
        back = affine(dx3_ref[rows], back_gain4, back_mean4) - scaled(normal, back_normal4)
        d_mixed = jnp.where(valid, back + goal_ref[0, rows].astype(f32), 0.0)
        dx3_ref[rows] = d_mixed
        d_scale = d_scale + fold(pool3_ref[rows] * d_mixed)
        weighted = scale3 * d_mixed * share
        col3_ref[step_rows(k, 1)] = weighted + from_left(weighted) + from_right(weighted)
        return d_scale

    acc_three[3] += sweep(unmix3, nothing3)
    normal3 = (spread(scaling3, WIDE), spread(-mean3 * scaling3, WIDE))

    def unpool3(k, carry):
        d_shift, d_gain = carry
        rows = step_rows(k)
        valid = widen(inv3_ref[rows]) > 0.0
        d_normal = jnp.where(valid, row_windows3(k) - scale3 * dx3_ref[rows], 0.0)
        pool3_ref[rows] = d_normal
        normal = affine(e_ref[rows], *normal3)
        return (d_shift + fold(d_normal), d_gain + fold(d_normal * normal))

    d_shift, d_gain = sweep(unpool3, (nothing3, nothing3))
    acc_three[2] += d_shift
    acc_three[1] += d_gain
    mean_shift = by_image(d_shift * gain3) / count_three
    mean_gain = by_image(d_gain * gain3) / count_three
    back_gain3 = scaling3 * gain3
    back_mean3 = spread(-scaling3 * mean_shift, WIDE)
    back_normal3 = spread(scaling3 * mean_gain, WIDE)

    def unnorm3(k, d_bias):
        rows = step_rows(k)
        valid = widen(inv3_ref[rows]) > 0.0
        normal = affine(e_ref[rows], *normal3)
        back = affine(pool3_ref[rows], back_gain3, back_mean3) - scaled(normal, back_normal3)
        low = jnp.where(valid, dx3_ref[rows] + back, 0.0).astype(bf16)
        dpre_ref[rows] = low
        return d_bias + fold(low.astype(f32))

    acc_three[0] += sweep(unnorm3, nothing3)
    keep(gwe_ref, product_tn(patch_ref[...], dpre_ref[...]))
    dpatch_ref[0:AREA] = product_nt(dpre_ref[...], we_ref[...])
    dpatch_ref[AREA : AREA + LINE] = jnp.zeros((LINE, 9 * C2), f32)

    def gather_back(k, carry):
        rows = step_rows(k)

        def tap(ky, kx, source):
            at = (3 * ky + kx) * C2
            value = dpatch_ref[source, at : at + C2]
            if ky != kx:
                at = (3 * kx + ky) * C2
                value = jnp.where(flipped, dpatch_ref[source, at : at + C2], value)
            return value

        sources = []
        for ky in range(3):
            source = step_rows(k, 1 if ky == 0 else 0)
            sources.append(
                (tap(ky, 1, source), tap(ky, 2, source) + from_right(tap(ky, 0, source)))
            )
        for pc in range(2):
            for pr, value in ((0, sources[1][pc]), (1, sources[2][pc] + sources[0][pc])):
                plane = pr * 2 + pc
                valid = inv_ref[plane, rows] > 0.0
                back_ref[plane, rows] = jnp.where(valid, rounded(value), 0.0)
        return carry

    sweep(gather_back, 0)

    if pairs == 1:
        pack_blocks(range(2, 5))

    normal2 = (spread(scaling2, C2), spread(-mean2 * scaling2, C2))

    def begin_back(plane):
        low_goal = (scale2 * back_ref[plane]).astype(bf16)
        dy_ref[plane_rows(plane)] = low_goal
        hid_ref[plane % 2] = product_nt(low_goal, w2_ref[...])
        return fold(low_goal.astype(f32))

    d_out_bias = begin_back(0)
    d_shift, d_gain = nothing, nothing
    sums = [nothing] * (HID2 // 128)
    new_gw1, new_gw2 = None, None
    for plane in range(4):
        if plane < 3:
            d_out_bias = d_out_bias + begin_back(plane + 1)
        for k in range(STEPS):
            rows = step_rows(k)
            part = slice(plane * AREA + k * STEP, plane * AREA + k * STEP + STEP)
            for n, at in enumerate(range(0, HID2, 128)):
                lanes = slice(at, at + 128)
                low = g_ref[part, lanes].astype(f32) * hid_ref[plane % 2, rows, lanes]
                low = low.astype(bf16)
                g_ref[part, lanes] = low
                sums[n] = sums[n] + fold(low.astype(f32))
        flat = plane_rows(plane)
        d_low = product_nt(g_ref[flat], w1_ref[...])
        dx_ref[plane] = d_low
        d_shift = d_shift + fold(d_low)
        d_gain = d_gain + fold(d_low * affine(mix_ref[plane], *normal2))
        part_gw1 = product_tn(h_ref[flat], g_ref[flat])
        part_gw2 = product_tn(dy_ref[flat], u_ref[flat])
        new_gw1 = part_gw1 if plane == 0 else new_gw1 + part_gw1
        new_gw2 = part_gw2 if plane == 0 else new_gw2 + part_gw2
    new_gw2 = new_gw2.T
    for n, value in enumerate(sums):
        acc_hid_two[:, n * 128 : n * 128 + 128] += value
    acc_two[6] += d_out_bias
    acc_two[4] += d_shift
    acc_two[3] += d_gain
    mean_out[0, 0] = spread(by_image(d_shift * gain2) / count_two, 128)
    mean_out[0, 1] = spread(by_image(d_gain * gain2) / count_two, 128)
    keep(gw1_ref, new_gw1)
    keep(gw2_ref, new_gw2)
    d_scale = fold(w2_ref[...].astype(f32) * new_gw2) + out_bias * d_out_bias
    acc_two[5] += d_scale / scale2

    def finish():
        if pairs > 1:
            pack_blocks(range(5))
        else:
            pack_blocks(range(2))

        def filler(number, carry):
            put_block(number, jnp.zeros((HALF, 128), bf16))
            return carry

        lax.fori_loop(USED, slots, filler, 0)

        flat_ref[...] = jnp.zeros(flat_ref.shape, f32)

        def put(at, total, length):
            if at % 128:
                room = jnp.zeros((8, 128), f32)
                if total.shape[1] < length + BS:
                    total = jnp.concatenate([total, room], axis=1)
                total = pltpu.roll(total, BS, 1)
            whole = jnp.sum(total, axis=0, keepdims=True)
            done = -(at % 128)
            row = at // 128
            lane = 0
            while done < length:
                first = max(0, -done)
                last = min(128, length - done)
                flat_ref[row : row + 1, first:last] = whole[:, lane + first : lane + last]
                done += 128
                lane += 128
                row += 1

        at = 3 * C2
        for n in range(3, 6):
            put(at, acc_two[n], C2)
            at += C2
        put(at, acc_hid_two[...], HID2)
        at += HID2
        put(at, acc_two[6], C2)
        at += C2
        for n in range(7):
            put(at, acc_three[n], C3)
            at += C3
        put(at, acc_hid_three[...], HID3)
        at += HID3
        put(at, acc_three[7], C3)

    at_pair(pairs - 1, finish)


def run_main(places, place, buckets, state, goal, vec, weights, strip_count):
    pairs = goal.shape[0]
    slots = places[0].shape[0]
    half = slots // 2 + 1
    if pairs == 1:
        state = held_in(pltpu.VMEM, *state)
    weights = held_in(pltpu.VMEM, *weights)
    _, inv, _, mix, stat = state
    state_shapes = [STATE[1], STATE[3], STATE[4]]
    grad_kind = bf16 if pairs == 1 else f32
    wide_f32 = pltpu.VMEM((AREA, WIDE), f32)
    wide_bf16 = pltpu.VMEM((AREA, WIDE), bf16)
    scratch = [
        pltpu.VMEM((4, AREA + LINE, C2), f32),
        pltpu.VMEM((2, AREA, HID2), f32),
        pltpu.VMEM((4 * AREA, HID2), bf16),
        pltpu.VMEM((4 * AREA, HID2), bf16),
        pltpu.VMEM((4 * AREA, C2), bf16),
        pltpu.VMEM((4 * AREA, C2), bf16),
        pltpu.VMEM((AREA, 9 * C2), bf16),
        pltpu.VMEM((AREA + LINE, 9 * C2), f32),
        pltpu.VMEM((AREA, 128), f32),
        wide_f32,
        pltpu.VMEM((AREA + 2 * LINE, WIDE), f32),
        wide_f32,
        wide_f32,
        wide_f32,
        pltpu.VMEM((AREA, HID3), f32),
        pltpu.VMEM((AREA, HID3), f32),
        pltpu.VMEM((AREA, HID3), bf16),
        pltpu.VMEM((AREA, HID3), bf16),
        wide_bf16,
        wide_bf16,
        wide_bf16,
        pltpu.VMEM((C2, HID2), grad_kind),
        pltpu.VMEM((HID2, C2), grad_kind),
        pltpu.VMEM((9 * C2, WIDE), grad_kind),
        pltpu.VMEM((WIDE, HID3), grad_kind),
        pltpu.VMEM((HID3, WIDE), grad_kind),
        pltpu.VMEM((7, 8, C2), f32),
        pltpu.VMEM((8, HID2), f32),
        pltpu.VMEM((8, 8, WIDE), f32),
        pltpu.VMEM((8, HID3), f32),
    ]
    out_shapes = [(half, HALF, 128), (half, HALF, 128), (VEC_BLOCKS * HALF, 128)]
    make = pltpu.VMEM if pairs == 1 else jax.ShapeDtypeStruct
    return pl.pallas_call(
        functools.partial(main_kernel, pairs, strip_count, slots),
        grid=() if pairs == 1 else (pairs,),
        in_specs=[SMEM] * 4
        + pair_specs(pairs, state_shapes + [goal.shape[1:]], pl.Buffered(1))
        + whole_specs(pairs, [vec.shape])
        + [VMEM_BLOCK] * 5,
        out_specs=pair_specs(pairs, [(AREA, WIDE)] + BACK) + whole_specs(pairs, out_shapes),
        out_shape=pair_arrays(pairs, [(AREA, WIDE)] + BACK, [f32] * 4)
        + [make(shape, kind) for shape, kind in zip(out_shapes, (bf16, bf16, f32))],
        scratch_shapes=scratch,
        compiler_params=pltpu.CompilerParams(
            vmem_limit_bytes=(40 if pairs == 1 else 56) * 1024 * 1024,
            fuse_transposed_lhs_in_matmul=True,
        ),
        name="blocks",
    )(*places, place, buckets, inv, mix, stat, goal, vec, *weights)


def exit_kernel(
    pairs,
    strip_count,
    place_ref,
    bucket_ref,
    x_in,
    inv_in,
    pool_in,
    mix_in,
    stat_in,
    zed_in,
    dx_in,
    mean_in,
    flat_ref,
    vec_ref,
    payload_hbm,
    vector_ref,
    payload_ref,
    image_ref,
    col_ref,
    dx_ref,
    back_ref,
    acc_ref,
    sem,
):
    pair = pl.program_id(0) if pairs > 1 else 0
    x_ref, inv_ref, pool_ref, mix_ref, stat_ref, zed_ref, low_ref, mean_ref = (
        ref.at[0] for ref in (x_in, inv_in, pool_in, mix_in, stat_in, zed_in, dx_in, mean_in)
    )
    bucket_of = bucket_reader(place_ref, bucket_ref, strip_count)
    shape = Geometry(bucket_of, pair)
    count_two = shape.count_two
    gain1, bias1, scale1, gain2 = (vec_ref[n : n + 1] for n in range(4))
    mean1, scaling1, mean2, scaling2 = (stat_ref[n] for n in range(4))
    normal2 = (scaling2, -mean2 * scaling2)
    clear_edges(col_ref)
    nothing = jnp.zeros((8, C2), f32)
    back_gain2 = scaling2 * gain2
    back_mean2 = -scaling2 * mean_ref[0]
    back_normal2 = scaling2 * mean_ref[1]

    if pairs > 1:

        @pl.when(pair == 0)
        def _():
            acc_ref[...] = jnp.zeros(acc_ref.shape, f32)

    def add_up(n, total):
        acc_ref[n] = total if pairs == 1 else acc_ref[n] + total

    def unmix(k, d_scale):
        rows = step_rows(k)
        for pr in range(2):
            weighted = []
            for pc in range(2):
                plane = pr * 2 + pc
                share = inv_ref[plane, rows]
                normal = affine(mix_ref[plane, rows], *normal2)
                back = affine(low_ref[plane, rows], back_gain2, back_mean2)
                back = back - scaled(normal, back_normal2)
                d_mixed = jnp.where(share > 0.0, zed_ref[plane, rows] + back, 0.0)
                dx_ref[plane, rows] = d_mixed
                d_scale = d_scale + fold(pool_ref[plane, rows] * d_mixed)
                weighted.append(scale1 * d_mixed * share)
            put_col_windows(col_ref, pr, k, *weighted)
        return d_scale

    add_up(2, sweep(unmix, nothing))
    normal1 = (spread(scaling1, C2), spread(-mean1 * scaling1, C2))

    def unpool(k, carry):
        d_shift, d_gain = carry
        rows = step_rows(k)
        for pc in range(2):
            windows = row_windows(col_ref, pc, k)
            for pr in range(2):
                plane = pr * 2 + pc
                valid = inv_ref[plane, rows] > 0.0
                d_normal = windows[pr] - scale1 * dx_ref[plane, rows]
                d_normal = jnp.where(valid, d_normal, 0.0)
                back_ref[plane, rows] = d_normal
                normal = affine(x_ref[plane, rows], *normal1)
                d_shift = d_shift + fold(d_normal)
                d_gain = d_gain + fold(d_normal * normal)
        return (d_shift, d_gain)

    d_shift, d_gain = sweep(unpool, (nothing, nothing))
    add_up(1, d_shift)
    add_up(0, d_gain)
    mean_shift = by_image(d_shift * gain1) / count_two
    mean_gain = by_image(d_gain * gain1) / count_two
    back_gain1 = scaling1 * gain1
    back_mean1 = spread(-scaling1 * mean_shift, C2)
    back_normal1 = spread(scaling1 * mean_gain, C2)

    def unnorm(k, carry):
        rows = step_rows(k)
        for plane in range(4):
            normal = affine(x_ref[plane, rows], *normal1)
            back = affine(back_ref[plane, rows], back_gain1, back_mean1)
            back = back - scaled(normal, back_normal1)
            valid = inv_ref[plane, rows] > 0.0
            dx_ref[plane, rows] = jnp.where(valid, dx_ref[plane, rows] + back, 0.0)
        return carry

    sweep(unnorm, 0)

    def give_back(plane, here, spot, there):
        image_ref[spot, there] = dx_ref[plane, here]

    image_ref[...] = jnp.zeros(image_ref.shape, f32)
    each_image(bucket_of, pair, give_back)

    for spot in range(2 * STRIPS):
        target = strip_place(pair, spot, strip_count)
        for within in range(SR):
            rows = slice(within * CW, within * CW + CW)
            payload_ref[target, within] = image_ref[spot, rows].astype(bf16)

    def finish():
        copy = pltpu.make_async_copy(payload_ref, payload_hbm, sem)
        copy.start()
        vector_ref[...] = flat_ref[...]
        for n in range(3):
            vector_ref[n : n + 1] = jnp.sum(acc_ref[n], axis=0, keepdims=True)
        copy.wait()

    if pairs == 1:
        finish()
    else:
        pl.when(pair == pairs - 1)(finish)


def run_exit(place, buckets, state, back, flat, vec, strip_count):
    pairs = strip_count // 8
    payload = (strip_count, SR, CW, C2)
    make = pltpu.VMEM if pairs == 1 else jax.ShapeDtypeStruct
    plane_f32 = pltpu.VMEM((4, AREA, C2), f32)
    arrays = [*state, *back]
    if pairs == 1:
        arrays = held_in(pltpu.VMEM, *arrays)
    return pl.pallas_call(
        functools.partial(exit_kernel, pairs, strip_count),
        grid=() if pairs == 1 else (pairs,),
        in_specs=[SMEM] * 2
        + pair_specs(pairs, STATE + BACK, pl.Buffered(1))
        + whole_specs(pairs, [flat.shape, vec.shape]),
        out_specs=[HBM] + whole_specs(pairs, [flat.shape]),
        out_shape=[pltpu.HBM(payload, bf16), make(flat.shape, f32)],
        scratch_shapes=[
            pltpu.VMEM(payload, bf16),
            pltpu.VMEM((2 * STRIPS, STRIP_ROWS, C2), f32),
            pltpu.VMEM((4, AREA + 2 * LINE, C2), f32),
            plane_f32,
            plane_f32,
            pltpu.VMEM((3, 8, C2), f32),
            pltpu.SemaphoreType.DMA,
        ],
        compiler_params=roomy(8 if pairs == 1 else 40),
        name="exit",
    )(place, buckets, *arrays, flat, vec)


def dense_blocks(values):
    return jnp.concatenate([values[:, :HALF], values[:, HALF:]], axis=2).astype(bf16)


def pack_kernel(master_ref, dense_ref):
    dense_ref[...] = dense_blocks(master_ref[...])


def pack(master):
    owned = master.shape[0]
    return pl.pallas_call(
        pack_kernel,
        out_shape=jax.ShapeDtypeStruct((owned, HALF, 2 * BS), bf16),
        name="pack",
    )(master)


def pack_pieces_kernel(place_ref, master_hbm, pixel_hbm, *refs):
    out_refs, (wide_ref, master_ref, pixel_ref, sem) = refs[:-4], refs[-4:]
    owned = master_ref.shape[0]
    slots = pixel_ref.shape[2]
    copies = [pltpu.make_async_copy(pixel_hbm, pixel_ref, sem.at[0])]
    parts = [(0, owned // 2), (owned // 2, owned - owned // 2)]
    for n, part in enumerate(parts):
        copies.append(
            pltpu.make_async_copy(
                master_hbm.at[pl.ds(*part)], master_ref.at[pl.ds(*part)], sem.at[1 + n]
            )
        )
    for copy in copies:
        copy.start()
    copies[0].wait()

    def widen_row(row, carry):
        start = pl.multiple_of(row * CW * slots, 8)
        values = pixel_ref[row].astype(f32).reshape(CW * slots, C2)
        wide_ref[pl.ds(start, CW * slots)] = values
        return carry

    lax.fori_loop(0, SR, widen_row, 0)
    for k, ref in enumerate(out_refs):
        for other in range(2):
            slot = place_ref[0] ^ (2 * k + other)
            first = other * (ref.shape[0] - STRIP_ROWS)
            strip = wide_ref[pl.ds(slot, STRIP_ROWS, stride=slots)]
            ref[first : first + STRIP_ROWS] = strip.astype(bf16)
    for (first, count), copy in zip(parts, copies[1:]):
        copy.wait()
        dense = dense_blocks(master_ref[first : first + count]).reshape(count * HALF, 2 * BS)
        start = STRIP_ROWS + first * HALF
        for ref in out_refs[:3]:
            ref[start : start + count * HALF] = dense


def pack_pieces(place, master, pixels):
    slots = pixels.shape[2]
    rows = master.shape[0] * HALF
    shapes = [(rows + 2 * STRIP_ROWS, 2 * BS)] * 3 + [(2 * STRIP_ROWS, 2 * BS)]
    return pl.pallas_call(
        pack_pieces_kernel,
        in_specs=[SMEM] + [HBM] * 2,
        out_specs=[VMEM_BLOCK] * 4,
        out_shape=[pltpu.VMEM(shape, bf16) for shape in shapes],
        scratch_shapes=[
            pltpu.VMEM((STRIP_ROWS * slots, C2), f32),
            pltpu.VMEM(master.shape, f32),
            pltpu.VMEM(pixels.shape, bf16),
            pltpu.SemaphoreType.DMA((3,)),
        ],
        compiler_params=roomy(12),
        name="pack",
    )(place, *held_in(pltpu.HBM, master, pixels))


def fold_pair_kernel(near_ref, got_ref, own_ref, *part_refs):
    share = own_ref.shape[0]

    def one(n, carry):
        own_ref[n] = near_ref[n].astype(f32) + got_ref[n].astype(f32)
        for k, ref in enumerate(part_refs):
            here = (k + 1) * share + n
            ref[n] = near_ref[here] + got_ref[here]
        return carry

    lax.fori_loop(0, share, one, 0, unroll=4)


def fold_pair(near, got, groups):
    shape = ((near.shape[0] - 1) // groups,) + near.shape[1:]
    return pl.pallas_call(
        fold_pair_kernel,
        in_specs=[VMEM_BLOCK] * 2,
        out_specs=[VMEM_BLOCK] * groups,
        out_shape=[pltpu.VMEM(shape, f32)] + [pltpu.VMEM(shape, bf16)] * (groups - 1),
        compiler_params=roomy(4),
        name="fold_pair",
    )(*held_in(pltpu.VMEM, near, got))


def fold_tile_kernel(pieces, spot_ref, *refs):
    piece_refs, refs = refs[:pieces], refs[pieces:]
    vector_refs, refs = refs[:pieces], refs[pieces:]
    out_refs, sum_ref = refs[:-1], refs[-1]
    groups = len(out_refs)
    share = out_refs[0].shape[0]
    owned = piece_refs[0].shape[0]
    total = vector_refs[0][...]
    for ref in vector_refs[1:]:
        total = total + ref[...]
    for n in range(sum_ref.shape[0]):
        sum_ref[n] = jnp.zeros((HALF, 128), f32)
    for n in range(VEC_BLOCKS):
        sum_ref[n] = total[n * HALF : (n + 1) * HALF]

    def one(n, carry):
        for k, out_ref in enumerate(out_refs):
            number = lax.rem(spot_ref[0] + k, groups) * share + n
            block = jnp.minimum(number, owned - 1)
            total = piece_refs[0][block].astype(f32)
            for ref in piece_refs[1:]:
                total = total + ref[block].astype(f32)
            rest = sum_ref[jnp.maximum(number - owned, 0)]
            out_ref[n] = jnp.where(number < owned, total, rest).astype(out_ref.dtype)
        return carry

    lax.fori_loop(0, share, one, 0, unroll=share <= 16)


def fold_tile(spot, pieces, vectors, extra, groups):
    shape = ((pieces[0].shape[0] + extra) // groups,) + pieces[0].shape[1:]
    return pl.pallas_call(
        functools.partial(fold_tile_kernel, len(pieces)),
        in_specs=[SMEM] + [VMEM_BLOCK] * (len(pieces) + len(vectors)),
        out_specs=[VMEM_BLOCK] * groups,
        out_shape=[pltpu.VMEM(shape, f32)] + [pltpu.VMEM(shape, bf16)] * (groups - 1),
        scratch_shapes=[pltpu.VMEM((extra, HALF, 128), f32)],
        compiler_params=roomy(8),
        name="fold_tile",
    )(spot, *held_in(pltpu.VMEM, *pieces, *vectors))


def fold_batch_kernel(owned, vector_weight, spot_ref, *refs):
    part_refs, (total_ref, norm_ref) = refs[:-2], refs[-2:]
    share = total_ref.shape[0]
    square = jnp.zeros((8, 128), f32)
    for n in range(share):
        total = part_refs[0][n].astype(f32)
        for ref in part_refs[1:]:
            total = total + ref[n].astype(f32)
        total_ref[n] = total.astype(bf16)
        weight = jnp.where(spot_ref[0] * share + n < owned, 1.0, vector_weight)
        square = square + weight * fold(total * total)
    square = jnp.sum(jnp.sum(square, axis=1, keepdims=True), axis=0, keepdims=True)
    norm_ref[...] = jnp.broadcast_to(square[None], norm_ref.shape)


def fold_batch(spot, parts, owned, tile_count):
    count = tile_count * len(parts)
    return pl.pallas_call(
        functools.partial(fold_batch_kernel, owned, 1.0 / tile_count),
        in_specs=[SMEM] + [VMEM_BLOCK] * len(parts),
        out_specs=[VMEM_BLOCK] * 2,
        out_shape=[pltpu.VMEM(parts[0].shape, bf16), pltpu.VMEM((count, 1, 128), f32)],
        name="fold_batch",
    )(spot, *held_in(pltpu.VMEM, *parts))


def update_kernel(owned, groups, spot_ref, norm_ref, *refs):
    quarters, refs = refs[:groups], refs[groups:]
    stat_hbm, out_hbm, (vector_ref, clip_ref), refs = refs[:5], refs[5:10], refs[10:12], refs[12:]
    stat_refs, out_refs, (in_sem, out_sem) = refs[:5], refs[5:10], refs[10:]
    master_ref, left_stat_ref, right_stat_ref, left_root_ref, right_root_ref = stat_refs
    grad_ref, left_ref, right_ref, new_ref, copy_ref = out_refs
    share = quarters[0].shape[0]
    spans = spans_of(owned)

    def copies_of(sources, targets, sems):
        return [
            [
                pltpu.make_async_copy(
                    source.at[pl.ds(*span)], target.at[pl.ds(*span)], sems.at[5 * n + k]
                )
                for k, (source, target) in enumerate(zip(sources, targets))
            ]
            for n, span in enumerate(spans)
        ]

    copies_in = copies_of(stat_hbm, stat_refs, in_sem)
    copies_out = copies_of(out_refs, out_hbm, out_sem)
    for copies in copies_in:
        for copy in copies:
            copy.start()
    norm = jnp.sqrt(jnp.sum(norm_ref[...], axis=0))
    factor = jnp.minimum(1.0, clip_limit / norm)
    left_half = lax.broadcasted_iota(jnp.int32, (HALF, 128), 1) < BS

    def summed(number):
        source = number // share
        local = number - source * share
        turn = lax.rem(spot_ref[0] - source + groups, groups)
        value = quarters[0][local].astype(f32)
        for k in range(1, groups):
            value = jnp.where(turn == k, quarters[k][local].astype(f32), value)
        return value * factor

    def side_by_side(first, count):
        sides = []
        for n in range(first, first + count, 2):
            dense = summed(n)
            turned = pltpu.roll(dense, BS, 1)
            if n + 1 < first + count:
                second = summed(n + 1)
                top = jnp.where(left_half, dense, pltpu.roll(second, BS, 1))
                low = jnp.where(left_half, turned, second)
                side = jnp.concatenate([top, low], axis=0)
                grad_ref[n + 1] = pltpu.roll(side, BS, 1)[:, :BS]
            else:
                side = jnp.concatenate([dense, turned], axis=0)[:, :BS]
            grad_ref[n] = side[:, :BS]
            sides.append(side.astype(bf16))
        return jnp.concatenate(sides, axis=1)

    def diagonal_of(count):
        order = (count * BS, count * BS)
        return lax.broadcasted_iota(jnp.int32, order, 0) // BS == (
            lax.broadcasted_iota(jnp.int32, order, 1) // BS
        )

    clip_ref[...] = norm
    for n in range(vector_ref.shape[0]):
        vector_ref[n] = summed(owned + n)
    for (first, length), arriving, leaving in zip(spans, copies_in, copies_out):
        parts = [(n, min(4, first + length - n)) for n in range(first, first + length, 4)]
        wides = [side_by_side(*part) for part in parts]
        tall = [
            jnp.where(diagonal_of(count), jnp.concatenate([wide] * count, axis=0), 0.0)
            for (_, count), wide in zip(parts, wides)
        ]
        lefts = [product_nt(one, wide) for one, wide in zip(tall, wides)]
        rights = [product_tn(wide, wide) for wide in wides]
        for copy in arriving:
            copy.wait()
        stepped = []
        for (start, count), wide in zip(parts, wides):
            roots = left_root_ref[pl.ds(start, count)].reshape(count * BS, BS).astype(bf16)
            stepped.append(product(roots, wide))
        for (start, count), left, right in zip(parts, lefts, rights):
            here = pl.ds(start, count)
            left_ref[here] = 0.5 * left_stat_ref[here] + 0.5 * left.reshape(count, BS, BS)
            for n in range(count):
                at = n // 2 * 128
                block = right[n * BS : n * BS + BS, at : min(at + 128, count * BS)]
                if n % 2:
                    block = pltpu.roll(block, BS, 1)
                right_ref[start + n] = 0.5 * right_stat_ref[start + n] + 0.5 * block[:, :BS]
        for (start, count), value in zip(parts, stepped):
            here = pl.ds(start, count)
            value = jnp.where(diagonal_of(count), value, 0.0).astype(bf16)
            roots = right_root_ref[here].reshape(count * BS, BS).astype(bf16)
            value = product(value, roots).reshape(count, BS, BS)
            new = master_ref[here] - rate_matrix * value
            new_ref[here] = new
            copy_ref[here] = new.astype(bf16)
        for copy in leaving:
            copy.start()
    for leaving in copies_out:
        for copy in leaving:
            copy.wait()


def spans_of(owned):
    spans = []
    first = 0
    while first < owned:
        length = min(8 if first == 0 else 12, owned - first)
        spans.append((first, length))
        first += length
    return spans


def update(spot, norm, quarters, extra, *stats):
    shape = stats[0].shape
    groups = len(quarters)
    types = [f32] * 4 + [bf16]
    steps = len(spans_of(shape[0]))
    return pl.pallas_call(
        functools.partial(update_kernel, shape[0], groups),
        in_specs=[SMEM] + [VMEM_BLOCK] * (groups + 1) + [HBM] * 5,
        out_specs=[HBM] * 5 + [VMEM_BLOCK] * 2,
        out_shape=[pltpu.HBM(shape, kind) for kind in types]
        + [
            pltpu.VMEM((extra, HALF, 128), f32),
            pltpu.VMEM((1, 128), f32),
        ],
        scratch_shapes=[pltpu.VMEM(shape, f32)] * 5
        + [pltpu.VMEM(shape, kind) for kind in types]
        + [
            pltpu.SemaphoreType.DMA((5 * steps,)),
            pltpu.SemaphoreType.DMA((5 * steps,)),
        ],
        compiler_params=roomy(20),
        name="update",
    )(spot, *held_in(pltpu.VMEM, norm, *quarters), *held_in(pltpu.HBM, *stats))


def share_out(pieces, axis):
    return lax.all_to_all(pieces, axis, split_axis=0, concat_axis=0, tiled=True)


def swap(piece, distance):
    count = lax.axis_size("tile")
    return lax.ppermute(piece, "tile", [(i, i ^ distance) for i in range(count)])


def on_device(
    pixels,
    buckets,
    slot_owner_table,
    out_grad,
    master,
    left_stat,
    right_stat,
    left_root,
    right_root,
    vectors,
    moment,
):
    tile_count = lax.axis_size("tile")
    tile_place = lax.axis_index("tile")
    slot_count = pixels.shape[2]
    group_count = tile_count // STRIPS
    pairs = group_count // 2
    owned = master.shape[0]
    slots = owned * tile_count
    batch_count = lax.axis_size("batch")
    spot = lax.axis_index("batch").astype(jnp.int32).reshape(1)
    extra = extra_of(owned, batch_count)
    place = tile_place.astype(jnp.int32).reshape(1)
    paired = tile_count == 8
    numbers = jnp.arange(slots, dtype=jnp.int32)
    slot_of = jnp.sum(
        jnp.where(slot_owner_table[None, :] == numbers[:, None], numbers[None, :], 0), axis=1
    )
    if paired:
        owner = slot_of // owned
        apart = owner ^ tile_place
        apart = (apart & 1) * (tile_count // 2) + (apart >> 1)
        slot_of = slot_of + owned * (apart - owner)
    half = slots // 2
    near_place = jnp.where(slot_of < half, slot_of, half)
    far_place = jnp.where(slot_of < half, half, slot_of - half)
    vec = vectors.reshape(-1, 128)
    turned = lax.dynamic_index_in_dim(
        buckets.reshape(group_count, slot_count), tile_place, 1, keepdims=False
    ) >= 2
    flips = turned.reshape(-1, 1, 1, 1)
    goal = out_grad.reshape(2 * pairs, H3, W3, C3)
    goal = jnp.where(flips, goal.transpose(0, 2, 1, 3), goal)[:, :LINES]
    goal = goal.reshape(pairs, 2, LINES, W3, C3).transpose(0, 2, 3, 1, 4)
    goal = goal.reshape(pairs, LINES, 2 * W3, C3)
    goal = jnp.pad(goal, ((0, 0), (0, 0), (0, LINE - 2 * W3), (0, WIDE - C3)))
    goal = goal.reshape(pairs, AREA, WIDE)

    if paired:
        own, for_x, for_y, for_both = pack_pieces(
            place, master, pixels[0, 0].transpose(1, 2, 0, 3)
        )
        goal, vec, slot_of, near_place, far_place, for_both = lax.optimization_barrier(
            (goal, vec, slot_of, near_place, far_place, for_both)
        )
        from_x, from_y, strips_both = swap(for_x, 2), swap(for_y, 4), swap(for_both, 6)
        near_half = (owned + 1) // 2
        middle = STRIP_ROWS + near_half * HALF
        first_half = swap(from_x[STRIP_ROWS:middle], 4)
        second_half = swap(from_y[middle : STRIP_ROWS + owned * HALF], 2)
        mine = [own, from_x, from_y, strips_both]
        theirs = [swap(piece, 1) for piece in mine]
        state = run_entry(place, buckets, mine + theirs, vec, tile_count)
        *state, first_half = lax.optimization_barrier((*state, first_half))
        pieces = mine[:3] + [first_half, second_half]
        pieces += theirs[:3] + [swap(first_half, 1), swap(second_half, 1)]
        spans = [(STRIP_ROWS, owned)] * 3 + [(0, near_half), (0, owned - near_half)]
        spans = spans * 2
    else:
        pieces = [lax.all_gather(pack(master), "tile", axis=0, tiled=True).reshape(-1, 2 * BS)]
        spans = [(0, slots)]
        strips = share_out(pixels.reshape(tile_count, STRIP, C2), "tile")
        strips = [jnp.pad(strips, ((0, 0), (0, STRIP_ROWS - STRIP), (0, 0)))]
        state = run_entry(place, buckets, strips, vec, tile_count)

    weights = run_unpack(slot_of, pieces, spans)
    result, *back, near, far, flat = run_main(
        (near_place, far_place),
        place,
        buckets,
        state,
        goal,
        vec,
        weights,
        tile_count,
    )
    pixel_back, vector = run_exit(place, buckets, state, back, flat, vec, tile_count)
    if paired:
        own, *parts = fold_pair(near, swap(far, 1), tile_count // 2)
        pieces = [own] + [swap(part, 2 * k + 2) for k, part in enumerate(parts)]
        vector, _ = lax.optimization_barrier((vector, parts[0]))
        vector = vector + swap(vector, 1)
        vectors_in = [vector] + [swap(vector, 2 * k) for k in range(1, tile_count // 2)]
    else:
        outgoing = jnp.concatenate([near[:half], far[:half]], axis=0)
        pieces = list(share_out(outgoing.reshape(tile_count, owned, HALF, 128), "tile"))
        vectors_in = list(lax.all_gather(vector, "tile"))
    result, pieces[1] = lax.optimization_barrier((result, pieces[1]))
    result = result.reshape(pairs, LINES, LINE, WIDE)[:, :, : 2 * W3, :C3]
    result = result.reshape(pairs, LINES, W3, 2, C3).transpose(0, 3, 1, 2, 4)
    result = result.reshape(2 * pairs, LINES, W3, C3)
    result = jnp.pad(result, ((0, 0), (0, H3 - LINES), (0, 0), (0, 0)))
    result = jnp.where(flips, result.transpose(0, 2, 1, 3), result)
    result = result.reshape(out_grad.shape)
    result = with_layout_constraint(result, Layout(major_to_minor=(0, 1, 2, 4, 5, 3, 6)))
    result, vectors_in[0] = lax.optimization_barrier((result, vectors_in[0]))
    own, *parts = fold_tile(spot, pieces, vectors_in, extra, batch_count)
    pixel_back, parts[0] = lax.optimization_barrier((pixel_back, parts[0]))
    returned = share_out(pixel_back, "tile")
    parts = [
        lax.ppermute(part, "batch", [(i, (i + k + 1) % batch_count) for i in range(batch_count)])
        for k, part in enumerate(parts)
    ]
    quarter, norm = fold_batch(spot, [own] + parts, owned, tile_count)
    returned, norm = lax.optimization_barrier((returned, norm))
    norm = share_out(norm, ("batch", "tile"))
    returned = returned.astype(f32).reshape(pixels.shape)
    returned = with_layout_constraint(returned, Layout(major_to_minor=(0, 1, 3, 4, 2, 5)))
    returned, quarter = lax.optimization_barrier((returned, quarter))
    quarters = [quarter] + [
        lax.ppermute(quarter, "batch", [(i, (i + k) % batch_count) for i in range(batch_count)])
        for k in range(1, batch_count)
    ]
    block_grad, left_new, right_new, master_new, weight_copy, whole_vector, clip = update(
        spot, norm, quarters, extra, master, left_stat, right_stat, left_root, right_root
    )
    clip_norm = clip[0, 0]
    share = vectors.shape[0] // tile_count
    whole_vector = whole_vector.reshape(-1)
    vec_grad = lax.dynamic_slice_in_dim(whole_vector, tile_place * share, share, 0)
    vec_moment = moment + vec_grad * vec_grad
    own_vectors = lax.dynamic_slice_in_dim(vectors, tile_place * share, share, 0)
    vec_new = own_vectors - rate_vector * vec_grad / (jnp.sqrt(vec_moment) + eps_adagrad)
    return (
        result,
        returned,
        clip_norm,
        block_grad,
        left_new,
        right_new,
        master_new,
        weight_copy,
        vec_grad,
        vec_moment,
        vec_new,
    )


def solution(mesh):
    placed = (
        P("batch", "tile", None, None, None, None),
        P("batch"),
        P(),
        P("batch", "tile", None, None, None, None, None),
        P("tile", None, None),
        P("tile", None, None),
        P("tile", None, None),
        P("tile", None, None),
        P("tile", None, None),
        P(),
        P("tile"),
    )
    return jax.shard_map(
        on_device,
        mesh=mesh,
        in_specs=placed,
        out_specs=(
            P("batch", "tile", None, None, None, None, None),
            P("batch", "tile", None, None, None, None),
            P(),
            P("tile", None, None),
            P("tile", None, None),
            P("tile", None, None),
            P("tile", None, None),
            P("tile", None, None),
            P("tile"),
            P("tile"),
            P("tile"),
        ),
        check_vma=False,
    )
```

```python
import functools

import jax
import jax.numpy as jnp
from jax import lax
from jax.experimental import pallas as pl
from jax.experimental.layout import Layout, with_layout_constraint
from jax.experimental.pallas import tpu as pltpu
from jax.sharding import PartitionSpec as P

C2 = 128
HID2 = 512
C3 = 320
HID3 = 1280
CH = 36
CW = 36
STRIPS = 4
BS = 64
SR = CH // STRIPS
H3 = CH // 2
W3 = CW // 2
LONG = 7 * CH // 9
LINES = LONG // 2
WIDE = 384
LINE = 40
AREA = LINES * LINE
STEP = 2 * LINE
STEPS = AREA // STEP
HALF = BS // 2
STRIP = SR * CW
STRIP_ROWS = STRIP + -STRIP % 16

eps_norm = 1e-05
clip_limit = 1.0
rate_matrix = 0.3
rate_vector = 0.3
eps_adagrad = 1e-08
f32 = jnp.float32
bf16 = jnp.bfloat16

SHAPES = [(C2, HID2), (HID2, C2), (9 * C2, C3), (C3, HID3), (HID3, C3)]
USED = sum(rows // BS * (cols // BS) for rows, cols in SHAPES)
VEC_ROWS = (6 * C2 + HID2 + C2 + C3 + 6 * C3 + HID3 + C3) // 128


VEC_BLOCKS = -(-VEC_ROWS // HALF)


def extra_of(owned, groups):
    return VEC_BLOCKS + -(owned + VEC_BLOCKS) % groups


def product(left, right):
    return jnp.dot(left, right, preferred_element_type=f32)


def product_nt(left, right):
    return lax.dot_general(left, right, (((1,), (1,)), ((), ())), preferred_element_type=f32)


def product_tn(left, right):
    return lax.dot_general(left, right, (((0,), (0,)), ((), ())), preferred_element_type=f32)


def gelu_pair(values):
    bell = jnp.exp2(values * values * (-0.5 * 1.4426950408889634))
    step = pl.reciprocal(1.0 + (0.3275911 * 0.7071067811865476) * jnp.abs(values), approx=True)
    tail = step * (
        0.5 * 0.254829592
        + step
        * (
            0.5 * -0.284496736
            + step
            * (0.5 * 1.421413741 + step * (0.5 * -1.453152027 + step * (0.5 * 1.061405429)))
        )
    )
    tail = tail * bell
    share = jnp.where(values >= 0.0, 1.0 - tail, tail)
    return (values * share, share + values * (bell * 0.3989422804014327))


def fold(values):
    chans = values.shape[-1]
    return jnp.sum(values.reshape(-1, 8, chans), axis=0)


def by_image(total):
    total = total + pltpu.roll(total, 4, 0)
    total = total + pltpu.roll(total, 2, 0)
    return jnp.sum(total, axis=1, keepdims=True)


def line(pattern):
    return jnp.concatenate([pattern] * (LINE // 8), axis=0)


def spread(pattern, chans):
    return jnp.broadcast_to(pattern, (8, chans))


def affine(values, factor, shift):
    tiles = values.reshape(-1, 8, values.shape[-1])
    return (tiles * factor + shift).reshape(values.shape)


def scaled(values, factor):
    tiles = values.reshape(-1, 8, values.shape[-1])
    return (tiles * factor).reshape(values.shape)


def from_left(values):
    return pltpu.roll(values, 2, 0)


def from_right(values):
    return pltpu.roll(values, values.shape[0] - 2, 0)


def rounded(values):
    return values.astype(bf16).astype(f32)


def widen(values):
    return jnp.concatenate([values] * (WIDE // 128), axis=-1)


def norm_terms(total, square, count):
    mean = by_image(total) / count
    scaling = lax.rsqrt(by_image(square) / count - mean * mean + eps_norm)
    return (mean, scaling)


def sweep(visit, start):
    return lax.fori_loop(0, STEPS, visit, start, unroll=True)


def step_rows(k, lines=0):
    start = k * STEP + lines * LINE
    return pl.ds(start if isinstance(k, int) else pl.multiple_of(start, LINE), STEP)


def held_in(space, *arrays):
    return [pltpu.with_memory_space_constraint(array, space) for array in arrays]


VMEM_BLOCK = pl.BlockSpec(memory_space=pltpu.VMEM)
HBM = pl.BlockSpec(memory_space=pltpu.HBM)
SMEM = pl.BlockSpec(memory_space=pltpu.SMEM)


def roomy(mebibytes):
    return pltpu.CompilerParams(vmem_limit_bytes=mebibytes * 1024 * 1024)


def image_shape(bucket_of, pair, image):
    bucket = bucket_of(2 * pair + image)
    plain = jnp.where(bucket == 0, 5 * CH // 9, 7 * CH // 9)
    across = jnp.where(bucket == 0, CW, 7 * CW // 9)
    turned = (bucket >= 2).astype(jnp.int32)
    return (
        jnp.where(turned > 0, 5 * CW // 9, plain),
        jnp.where(turned > 0, CH, across),
        turned,
    )


def bucket_reader(place_ref, bucket_ref, strip_count):
    return lambda group: bucket_ref[group * strip_count + place_ref[0]]


class Geometry:
    def __init__(self, bucket_of, pair):
        parity = lax.broadcasted_iota(jnp.int32, (8, 128), 0) % 2
        even, odd = (image_shape(bucket_of, pair, image) for image in range(2))
        high, broad, turned = (jnp.where(parity == 0, a, b) for a, b in zip(even, odd))
        self.high = high
        self.count_two = (high * broad * C2).astype(f32)[:, :1]
        self.high3 = (high + 1) // 2
        broad3 = (broad + 1) // 2
        self.count_three = (self.high3 * broad3 * C3).astype(f32)[:, :1]
        place = lax.broadcasted_iota(jnp.int32, (LINE, 128), 0) // 2
        inside = lax.broadcasted_iota(jnp.int32, (LINE, 128), 0) < 2 * W3
        self.reach = []
        self.col_share = []
        for pc in range(2):
            column = 2 * place + pc
            self.reach.append(jnp.where(inside & (column < line(broad)), line(high), 0))
            edge = (column == 0) | (column == line(broad) - 1)
            self.col_share.append(jnp.where(edge, 0.5, 1.0 / 3.0))
        self.reach3 = jnp.where(inside & (place < line(broad3)), line(self.high3), 0)
        edge3 = (place == 0) | (place == line(broad3) - 1)
        self.col_share3 = jnp.where(edge3, 0.5, 1.0 / 3.0)
        self.flipped = jnp.concatenate([turned] * (STEP // 8), axis=0) > 0

    def share(self, plane, k):
        pr, pc = plane // 2, plane % 2
        return self.lines(4 * k + pr, 2, self.reach[pc], self.col_share[pc], self.high)

    def share3(self, k):
        return self.lines(2 * k, 1, self.reach3, self.col_share3, self.high3)

    def lines(self, row, stride, reach, col_share, height):
        parts = []
        for n in range(2):
            here = row + stride * n
            row_share = jnp.where((here == 0) | (here == height - 1), 0.5, 1.0 / 3.0)
            parts.append(jnp.where(here < reach, line(row_share) * col_share, 0.0))
        return jnp.concatenate(parts, axis=0)


def strip_place(pair, spot, strip_count):
    return lax.rem(pair * 8 + strip_count - 2 + spot, strip_count)


def each_image(bucket_of, pair, visit):
    for image in range(2):
        way = image_shape(bucket_of, pair, image)[2]

        @pl.when(way == 0)
        def _():
            def one(r, carry):
                for plane in range(4):
                    row = 2 * r + plane // 2
                    strip = row // SR
                    there = pl.ds((row - strip * SR) * CW + plane % 2, W3, stride=2)
                    here = pl.ds(r * LINE + image, W3, stride=2)
                    visit(plane, here, image * STRIPS + strip, there)
                return carry

            lax.fori_loop(0, LINES, one, 0)

        @pl.when(way == 1)
        def _():
            def one(r, carry):
                for plane in range(4):
                    for strip in range(STRIPS):
                        first = (plane % 2 + strip * SR) % 2
                        count = (SR - first + 1) // 2
                        done = (strip * SR + first) // 2
                        column = 2 * r + plane // 2
                        there = pl.ds(first * CW + column, count, stride=2 * CW)
                        here = pl.ds(r * LINE + image + 2 * done, count, stride=2)
                        visit(plane, here, image * STRIPS + strip, there)
                return carry

            lax.fori_loop(0, LINES, one, 0)


def row_windows(col_ref, pc, k):
    both = col_ref[pc, step_rows(k, 1)] + col_ref[2 + pc, step_rows(k, 1)]
    return (both + col_ref[2 + pc, step_rows(k)], both + col_ref[pc, step_rows(k, 2)])


def put_col_windows(col_ref, pr, k, even, odd):
    both = even + odd
    col_ref[pr * 2, step_rows(k, 1)] = both + from_left(odd)
    col_ref[pr * 2 + 1, step_rows(k, 1)] = both + from_right(even)


def clear_edges(col_ref):
    zero_line = jnp.zeros((LINE, C2), f32)
    for plane in range(4):
        col_ref[plane, 0:LINE] = zero_line
        col_ref[plane, AREA + LINE : AREA + 2 * LINE] = zero_line


def entry_kernel(pairs, strip_count, piece_count, place_ref, bucket_ref, vec_ref, *refs):
    piece_refs, refs = refs[:piece_count], refs[piece_count:]
    x_out, inv_out, pool_out, mix_out, stat_out, image_ref, col_ref = refs
    pair = pl.program_id(0) if pairs > 1 else 0
    x_ref, inv_ref, pool_ref, mix_ref = (ref.at[0] for ref in (x_out, inv_out, pool_out, mix_out))
    bucket_of = bucket_reader(place_ref, bucket_ref, strip_count)
    shape = Geometry(bucket_of, pair)
    gain1, bias1, scale1 = (vec_ref[n : n + 1] for n in range(3))
    clear_edges(col_ref)
    if piece_count > 1:
        half = piece_count // 2
        for n, ref in enumerate(piece_refs):
            source = place_ref[0] ^ (n // half + 2 * (n % half))
            spot = lax.rem(source + 2, 2 * STRIPS)
            first = 0 if n < half else ref.shape[0] - STRIP_ROWS
            image_ref[spot] = ref[first : first + STRIP_ROWS].astype(f32)
    else:
        for spot in range(2 * STRIPS):
            source = strip_place(pair, spot, strip_count)
            image_ref[spot] = piece_refs[0][source].astype(f32)

    def take_in(plane, here, spot, there):
        x_ref[plane, here] = image_ref[spot, there]

    each_image(bucket_of, pair, take_in)

    def arrange(k, carry):
        total, square = carry
        rows = step_rows(k)
        for plane in range(4):
            share = shape.share(plane, k)
            inv_ref[plane, rows] = share
            values = jnp.where(share > 0.0, x_ref[plane, rows], 0.0)
            x_ref[plane, rows] = values
            total = total + fold(values)
            square = square + fold(values * values)
        return (total, square)

    nothing = jnp.zeros((8, C2), f32)
    total, square = sweep(arrange, (nothing, nothing))
    mean1, scaling1 = norm_terms(total, square, shape.count_two)
    factor1 = scaling1 * gain1
    shift1 = bias1 - mean1 * scaling1 * gain1

    def window_cols(k, carry):
        rows = step_rows(k)
        for pr in range(2):
            masked = []
            for pc in range(2):
                plane = pr * 2 + pc
                normal = rounded(affine(x_ref[plane, rows], factor1, shift1))
                masked.append(jnp.where(inv_ref[plane, rows] > 0.0, normal, 0.0))
            put_col_windows(col_ref, pr, k, *masked)
        return carry

    sweep(window_cols, 0)

    def mix(k, carry):
        total, square = carry
        rows = step_rows(k)
        for pc in range(2):
            windows = row_windows(col_ref, pc, k)
            for pr in range(2):
                plane = pr * 2 + pc
                values = x_ref[plane, rows]
                share = inv_ref[plane, rows]
                pooled = windows[pr] * share - rounded(affine(values, factor1, shift1))
                pooled = jnp.where(share > 0.0, pooled, 0.0)
                mixed = values + scale1 * pooled
                pool_ref[plane, rows] = pooled
                mix_ref[plane, rows] = mixed
                total = total + fold(mixed)
                square = square + fold(mixed * mixed)
        return (total, square)

    total, square = sweep(mix, (nothing, nothing))
    mean2, scaling2 = norm_terms(total, square, shape.count_two)
    for n, value in enumerate((mean1, scaling1, mean2, scaling2)):
        stat_out[0, n] = spread(value, 128)


def pair_specs(pairs, shapes, mode=None):
    if pairs == 1:
        return [VMEM_BLOCK] * len(shapes)
    return [
        pl.BlockSpec(
            (1,) + shape, lambda t, rank=len(shape): (t,) + (0,) * rank, pipeline_mode=mode
        )
        for shape in shapes
    ]


def whole_specs(pairs, shapes):
    if pairs == 1:
        return [VMEM_BLOCK] * len(shapes)
    return [
        pl.BlockSpec(
            shape,
            lambda t, rank=len(shape): (0,) * rank,
            pipeline_mode=pl.Buffered(1),
        )
        for shape in shapes
    ]


def pair_arrays(pairs, shapes, kinds):
    make = pltpu.VMEM if pairs == 1 else jax.ShapeDtypeStruct
    return [make((pairs,) + shape, kind) for shape, kind in zip(shapes, kinds)]


STATE = [(4, AREA, C2)] * 4 + [(4, 8, 128)]
BACK = [(4, AREA, C2)] * 2 + [(2, 8, 128)]


def run_entry(place, buckets, pieces, vec, strip_count):
    pairs = strip_count // 8
    if pairs == 1:
        pieces = held_in(pltpu.VMEM, *pieces)
    return pl.pallas_call(
        functools.partial(entry_kernel, pairs, strip_count, len(pieces)),
        grid=() if pairs == 1 else (pairs,),
        in_specs=[SMEM] * 2 + whole_specs(pairs, [array.shape for array in (vec, *pieces)]),
        out_specs=pair_specs(pairs, STATE),
        out_shape=pair_arrays(pairs, STATE, [f32] * 5),
        scratch_shapes=[
            pltpu.VMEM((2 * STRIPS, STRIP_ROWS, C2), f32),
            pltpu.VMEM((4, AREA + 2 * LINE, C2), f32),
        ],
        compiler_params=roomy(6 if pairs == 1 else 40),
        name="entry",
    )(place, buckets, vec, *pieces)


WEIGHTS = [(C2, HID2), (HID2, C2), (9 * C2, WIDE), (WIDE, HID3), (HID3, WIDE)]


def unpack_kernel(spans, slot_ref, *refs):
    piece_refs, refs = refs[: len(spans)], refs[len(spans) :]
    weights, gathered_ref = refs[:-1], refs[-1]
    done = 0
    for ref, (first, count) in zip(piece_refs, spans):
        blocks = ref[first : first + count * HALF].reshape(count, HALF, 128)
        gathered_ref[done : done + count] = blocks
        done += count
    left_half = lax.broadcasted_iota(jnp.int32, (HALF, 128), 1) < BS
    offset = 0
    for (rows, cols), ref in zip(SHAPES, weights):
        wide = cols // BS
        for rb in range(rows // BS):
            for cb in range(0, wide, 2):
                number = offset + rb * wide + cb
                first = gathered_ref[slot_ref[number]]
                turned = pltpu.roll(first, BS, 1)
                if cb + 1 < wide:
                    second = gathered_ref[slot_ref[number + 1]]
                    top = jnp.where(left_half, first, pltpu.roll(second, BS, 1))
                    low = jnp.where(left_half, turned, second)
                else:
                    top = jnp.where(left_half, first, 0.0)
                    low = jnp.where(left_half, turned, 0.0)
                place = slice(cb * BS, cb * BS + 128)
                ref[rb * BS : rb * BS + HALF, place] = top
                ref[rb * BS + HALF : rb * BS + BS, place] = low
        offset += rows // BS * wide
    weights[3][C3:, :] = jnp.zeros((WIDE - C3, HID3), bf16)


def run_unpack(slot_of, pieces, spans):
    slots = slot_of.shape[0]
    return pl.pallas_call(
        functools.partial(unpack_kernel, spans),
        in_specs=[SMEM] + [VMEM_BLOCK] * len(pieces),
        out_specs=[VMEM_BLOCK] * 5,
        out_shape=[pltpu.VMEM(shape, bf16) for shape in WEIGHTS],
        scratch_shapes=[pltpu.VMEM((slots, HALF, 128), bf16)],
        compiler_params=roomy(6),
        name="unpack",
    )(slot_of, *held_in(pltpu.VMEM, *pieces))


def main_kernel(
    pairs,
    strip_count,
    slots,
    near_place,
    far_place,
    place_ref,
    bucket_ref,
    inv_in,
    mix_in,
    stat_in,
    goal_ref,
    vec_ref,
    w1_ref,
    w2_ref,
    we_ref,
    w3_ref,
    w4_ref,
    result_ref,
    zed_out,
    dx_out,
    mean_out,
    near_ref,
    far_ref,
    flat_ref,
    zed_ref,
    hid_ref,
    u_ref,
    g_ref,
    h_ref,
    dy_ref,
    patch_ref,
    dpatch_ref,
    inv3_ref,
    e_ref,
    col3_ref,
    pool3_ref,
    mix3_ref,
    dx3_ref,
    hid3_ref,
    dhid3_ref,
    u3_ref,
    g3_ref,
    h3_ref,
    dy3_ref,
    dpre_ref,
    gw1_ref,
    gw2_ref,
    gwe_ref,
    gw3_ref,
    gw4_ref,
    acc_two,
    acc_hid_two,
    acc_three,
    acc_hid_three,
):
    pair = pl.program_id(0) if pairs > 1 else 0
    grads = [gw1_ref, gw2_ref, gwe_ref, gw3_ref, gw4_ref]
    inv_ref, mix_ref, stat_ref = (ref.at[0] for ref in (inv_in, mix_in, stat_in))
    back_ref, dx_ref = zed_out.at[0], dx_out.at[0]
    left_half = lax.broadcasted_iota(jnp.int32, (HALF, 128), 1) < BS

    def at_pair(number, act):
        if pairs == 1:
            act()
        else:
            pl.when(pair == number)(act)

    def begin():
        acc_two[...] = jnp.zeros(acc_two.shape, f32)
        acc_hid_two[...] = jnp.zeros(acc_hid_two.shape, f32)
        acc_three[...] = jnp.zeros(acc_three.shape, f32)
        acc_hid_three[...] = jnp.zeros(acc_hid_three.shape, f32)

    at_pair(0, begin)
    shape = Geometry(bucket_reader(place_ref, bucket_ref, strip_count), pair)
    count_two, count_three, flipped = shape.count_two, shape.count_three, shape.flipped
    nothing = jnp.zeros((8, C2), f32)
    nothing3 = jnp.zeros((8, WIDE), f32)

    def vector_row(at, length):
        first, shift = at // 128, at % 128
        count = -(-(shift + length) // 128)
        row = jnp.concatenate([vec_ref[first + n : first + n + 1] for n in range(count)], axis=1)
        if shift:
            row = pltpu.roll(jnp.broadcast_to(row, (8, count * 128)), count * 128 - shift, 1)[:1]
        return row

    def wide_row(at):
        lane = lax.broadcasted_iota(jnp.int32, (1, WIDE), 1)
        return jnp.where(lane < C3, vector_row(at, C3)[:, :WIDE], 0.0)

    gain2, bias2, scale2 = (vec_ref[n : n + 1] for n in range(3, 6))
    hid_bias = vector_row(6 * C2, HID2)
    out_bias = vector_row(6 * C2 + HID2, C2)
    two = 7 * C2 + HID2
    embed_bias, gain3, bias3, scale3 = (wide_row(two + n * C3) for n in range(4))
    gain4, bias4, scale4 = (wide_row(two + n * C3) for n in range(4, 7))
    hid_bias3 = vector_row(two + 7 * C3, HID3)[:, :HID3]
    out_bias3 = wide_row(two + 7 * C3 + HID3)
    mean2, scaling2 = stat_ref[2], stat_ref[3]
    factor2 = scaling2 * gain2
    shift2 = bias2 - mean2 * scaling2 * gain2
    for plane in range(4):
        zed_ref[plane, 0:LINE] = jnp.zeros((LINE, C2), f32)
    col3_ref[0:LINE] = jnp.zeros((LINE, WIDE), f32)
    col3_ref[AREA + LINE : AREA + 2 * LINE] = jnp.zeros((LINE, WIDE), f32)

    def put_block(number, block):
        near_ref[near_place[number]] = block
        far_ref[far_place[number]] = block

    def pack_blocks(matrices):
        offsets = [0]
        for rows, cols in SHAPES:
            offsets.append(offsets[-1] + rows // BS * (cols // BS))
        for which in matrices:
            (rows, cols), ref = SHAPES[which], grads[which]
            wide = cols // BS
            for rb in range(rows // BS):
                for cb in range(0, wide, 2):
                    number = offsets[which] + rb * wide + cb
                    at = slice(cb * BS, cb * BS + 128)
                    top = ref[rb * BS : rb * BS + HALF, at].astype(bf16)
                    low = ref[rb * BS + HALF : rb * BS + BS, at].astype(bf16)
                    put_block(number, jnp.where(left_half, top, pltpu.roll(low, BS, 1)))
                    if cb + 1 < wide:
                        put_block(number + 1, jnp.where(left_half, pltpu.roll(top, BS, 1), low))

    def plane_rows(plane):
        return slice(plane * AREA, plane * AREA + AREA)

    def begin_plane(plane):
        low = affine(mix_ref[plane], factor2, shift2).astype(bf16)
        h_ref[plane_rows(plane)] = low
        hid_ref[plane % 2] = product(low, w1_ref[...])

    begin_plane(0)
    for plane in range(4):
        if plane < 3:
            begin_plane(plane + 1)
        for k in range(STEPS):
            rows = step_rows(k)
            flat = slice(plane * AREA + k * STEP, plane * AREA + k * STEP + STEP)
            for at in range(0, HID2, 128):
                lanes = slice(at, at + 128)
                active, slope = gelu_pair(hid_ref[plane % 2, rows, lanes] + hid_bias[:, lanes])
                u_ref[flat, lanes] = active.astype(bf16)
                g_ref[flat, lanes] = slope.astype(bf16)
        out = product(u_ref[plane_rows(plane)], w2_ref[...]) + out_bias
        zed = jnp.where(inv_ref[plane] > 0.0, mix_ref[plane] + scale2 * out, 0.0)
        zed_ref[plane, LINE : LINE + AREA] = rounded(zed)

    def patches(k, carry):
        rows = step_rows(k)
        taps = []
        for ky in range(3):
            pr = (0 if ky == 1 else 1) * 2
            source = step_rows(k, 0 if ky == 0 else 1)
            even = zed_ref[pr, source]
            odd = zed_ref[pr + 1, source]
            taps.append((from_left(odd), even, odd))
        for ky in range(3):
            for kx in range(3):
                at = (3 * ky + kx) * C2
                tap = taps[ky][kx]
                if ky != kx:
                    tap = jnp.where(flipped, taps[kx][ky], tap)
                patch_ref[rows, at : at + C2] = tap.astype(bf16)
        return carry

    sweep(patches, 0)
    e_ref[...] = product(patch_ref[...], we_ref[...])

    def embed(k, carry):
        total, square = carry
        rows = step_rows(k)
        share = shape.share3(k)
        inv3_ref[rows] = share
        out = jnp.where(widen(share) > 0.0, e_ref[rows] + embed_bias, 0.0)
        e_ref[rows] = out
        return (total + fold(out), square + fold(out * out))

    total, square = sweep(embed, (nothing3, nothing3))
    mean3, scaling3 = norm_terms(total, square, count_three)
    factor3 = scaling3 * gain3
    shift3 = bias3 - mean3 * scaling3 * gain3

    def window_cols3(k, carry):
        rows = step_rows(k)
        normal = rounded(affine(e_ref[rows], factor3, shift3))
        masked = jnp.where(widen(inv3_ref[rows]) > 0.0, normal, 0.0)
        col3_ref[step_rows(k, 1)] = masked + from_left(masked) + from_right(masked)
        return carry

    sweep(window_cols3, 0)

    def row_windows3(k):
        return col3_ref[step_rows(k)] + col3_ref[step_rows(k, 1)] + col3_ref[step_rows(k, 2)]

    def mix3(k, carry):
        total, square = carry
        rows = step_rows(k)
        values = e_ref[rows]
        share = widen(inv3_ref[rows])
        pooled = row_windows3(k) * share - rounded(affine(values, factor3, shift3))
        pooled = jnp.where(share > 0.0, pooled, 0.0)
        mixed = values + scale3 * pooled
        pool3_ref[rows] = pooled
        mix3_ref[rows] = mixed
        return (total + fold(mixed), square + fold(mixed * mixed))

    total, square = sweep(mix3, (nothing3, nothing3))
    mean4, scaling4 = norm_terms(total, square, count_three)
    factor4 = scaling4 * gain4
    shift4 = bias4 - mean4 * scaling4 * gain4
    normal4 = (spread(scaling4, WIDE), spread(-mean4 * scaling4, WIDE))

    def prepare3(k, d_bias):
        rows = step_rows(k)
        h3_ref[rows] = affine(mix3_ref[rows], factor4, shift4).astype(bf16)
        goal = goal_ref[0, rows].astype(f32)
        goal = jnp.where(widen(inv3_ref[rows]) > 0.0, goal, 0.0)
        low_goal = (scale4 * goal).astype(bf16)
        dy3_ref[rows] = low_goal
        return d_bias + fold(low_goal.astype(f32))

    acc_three[7] += sweep(prepare3, nothing3)

    def keep(ref, value, place=slice(None)):
        if pairs == 1:
            ref[place] = value.astype(ref.dtype)
        else:

            @pl.when(pair == 0)
            def _():
                ref[place] = value

            @pl.when(pair > 0)
            def _():
                ref[place] += value

    def begin_chunk(at):
        lanes = slice(at, at + 256)
        hid3_ref[:, lanes] = product(h3_ref[...], w3_ref[:, lanes])
        dhid3_ref[:, lanes] = product_nt(dy3_ref[...], w4_ref[lanes])

    begin_chunk(0)
    for at in range(0, HID3, 256):
        if at + 256 < HID3:
            begin_chunk(at + 256)
        for lane in (at, at + 128):
            lanes = slice(lane, lane + 128)
            total = nothing
            for k in range(STEPS):
                rows = step_rows(k)
                active, slope = gelu_pair(hid3_ref[rows, lanes] + hid_bias3[:, lanes])
                u3_ref[rows, lanes] = active.astype(bf16)
                low = (slope * dhid3_ref[rows, lanes]).astype(bf16)
                g3_ref[rows, lanes] = low
                total = total + fold(low.astype(f32))
            acc_hid_three[:, lanes] += total
        lanes = slice(at, at + 256)
        out = product(u3_ref[:, lanes], w4_ref[lanes])
        d_low = product_nt(g3_ref[:, lanes], w3_ref[:, lanes])
        result_ref[0] = out if at == 0 else result_ref[0] + out
        dx3_ref[...] = d_low if at == 0 else dx3_ref[...] + d_low
        keep(gw3_ref, product_tn(h3_ref[...], g3_ref[:, lanes]), (slice(None), lanes))
        keep(gw4_ref, product_tn(u3_ref[:, lanes], dy3_ref[...]), lanes)

    def finish3(k, carry):
        d_scale, d_shift, d_gain = carry
        rows = step_rows(k)
        valid = widen(inv3_ref[rows]) > 0.0
        mixed = mix3_ref[rows]
        out = jnp.where(valid, result_ref[0, rows] + out_bias3, 0.0)
        result_ref[0, rows] = mixed + scale4 * out
        d_scale = d_scale + fold(out * goal_ref[0, rows].astype(f32))
        d_low = dx3_ref[rows]
        normal = affine(mixed, *normal4)
        return (d_scale, d_shift + fold(d_low), d_gain + fold(d_low * normal))

    d_scale, d_shift, d_gain = sweep(finish3, (nothing3, nothing3, nothing3))
    acc_three[6] += d_scale
    acc_three[5] += d_shift
    acc_three[4] += d_gain
    mean_shift = by_image(d_shift * gain4) / count_three
    mean_gain = by_image(d_gain * gain4) / count_three
    back_gain4 = scaling4 * gain4
    back_mean4 = spread(-scaling4 * mean_shift, WIDE)
    back_normal4 = spread(scaling4 * mean_gain, WIDE)

    def unmix3(k, d_scale):
        rows = step_rows(k)
        share = widen(inv3_ref[rows])
        valid = share > 0.0
        normal = affine(mix3_ref[rows], *normal4)
        back = affine(dx3_ref[rows], back_gain4, back_mean4) - scaled(normal, back_normal4)
        d_mixed = jnp.where(valid, back + goal_ref[0, rows].astype(f32), 0.0)
        dx3_ref[rows] = d_mixed
        d_scale = d_scale + fold(pool3_ref[rows] * d_mixed)
        weighted = scale3 * d_mixed * share
        col3_ref[step_rows(k, 1)] = weighted + from_left(weighted) + from_right(weighted)
        return d_scale

    acc_three[3] += sweep(unmix3, nothing3)
    normal3 = (spread(scaling3, WIDE), spread(-mean3 * scaling3, WIDE))

    def unpool3(k, carry):
        d_shift, d_gain = carry
        rows = step_rows(k)
        valid = widen(inv3_ref[rows]) > 0.0
        d_normal = jnp.where(valid, row_windows3(k) - scale3 * dx3_ref[rows], 0.0)
        pool3_ref[rows] = d_normal
        normal = affine(e_ref[rows], *normal3)
        return (d_shift + fold(d_normal), d_gain + fold(d_normal * normal))

    d_shift, d_gain = sweep(unpool3, (nothing3, nothing3))
    acc_three[2] += d_shift
    acc_three[1] += d_gain
    mean_shift = by_image(d_shift * gain3) / count_three
    mean_gain = by_image(d_gain * gain3) / count_three
    back_gain3 = scaling3 * gain3
    back_mean3 = spread(-scaling3 * mean_shift, WIDE)
    back_normal3 = spread(scaling3 * mean_gain, WIDE)

    def unnorm3(k, d_bias):
        rows = step_rows(k)
        valid = widen(inv3_ref[rows]) > 0.0
        normal = affine(e_ref[rows], *normal3)
        back = affine(pool3_ref[rows], back_gain3, back_mean3) - scaled(normal, back_normal3)
        low = jnp.where(valid, dx3_ref[rows] + back, 0.0).astype(bf16)
        dpre_ref[rows] = low
        return d_bias + fold(low.astype(f32))

    acc_three[0] += sweep(unnorm3, nothing3)
    keep(gwe_ref, product_tn(patch_ref[...], dpre_ref[...]))
    dpatch_ref[0:AREA] = product_nt(dpre_ref[...], we_ref[...])
    dpatch_ref[AREA : AREA + LINE] = jnp.zeros((LINE, 9 * C2), f32)

    def gather_back(k, carry):
        rows = step_rows(k)

        def tap(ky, kx, source):
            at = (3 * ky + kx) * C2
            value = dpatch_ref[source, at : at + C2]
            if ky != kx:
                at = (3 * kx + ky) * C2
                value = jnp.where(flipped, dpatch_ref[source, at : at + C2], value)
            return value

        sources = []
        for ky in range(3):
            source = step_rows(k, 1 if ky == 0 else 0)
            sources.append(
                (tap(ky, 1, source), tap(ky, 2, source) + from_right(tap(ky, 0, source)))
            )
        for pc in range(2):
            for pr, value in ((0, sources[1][pc]), (1, sources[2][pc] + sources[0][pc])):
                plane = pr * 2 + pc
                valid = inv_ref[plane, rows] > 0.0
                back_ref[plane, rows] = jnp.where(valid, rounded(value), 0.0)
        return carry

    sweep(gather_back, 0)

    if pairs == 1:
        pack_blocks(range(2, 5))

    normal2 = (spread(scaling2, C2), spread(-mean2 * scaling2, C2))

    def begin_back(plane):
        low_goal = (scale2 * back_ref[plane]).astype(bf16)
        dy_ref[plane_rows(plane)] = low_goal
        hid_ref[plane % 2] = product_nt(low_goal, w2_ref[...])
        return fold(low_goal.astype(f32))

    d_out_bias = begin_back(0)
    d_shift, d_gain = nothing, nothing
    sums = [nothing] * (HID2 // 128)
    new_gw1, new_gw2 = None, None
    for plane in range(4):
        if plane < 3:
            d_out_bias = d_out_bias + begin_back(plane + 1)
        for k in range(STEPS):
            rows = step_rows(k)
            part = slice(plane * AREA + k * STEP, plane * AREA + k * STEP + STEP)
            for n, at in enumerate(range(0, HID2, 128)):
                lanes = slice(at, at + 128)
                low = g_ref[part, lanes].astype(f32) * hid_ref[plane % 2, rows, lanes]
                low = low.astype(bf16)
                g_ref[part, lanes] = low
                sums[n] = sums[n] + fold(low.astype(f32))
        flat = plane_rows(plane)
        d_low = product_nt(g_ref[flat], w1_ref[...])
        dx_ref[plane] = d_low
        d_shift = d_shift + fold(d_low)
        d_gain = d_gain + fold(d_low * affine(mix_ref[plane], *normal2))
        part_gw1 = product_tn(h_ref[flat], g_ref[flat])
        part_gw2 = product_tn(dy_ref[flat], u_ref[flat])
        new_gw1 = part_gw1 if plane == 0 else new_gw1 + part_gw1
        new_gw2 = part_gw2 if plane == 0 else new_gw2 + part_gw2
    new_gw2 = new_gw2.T
    for n, value in enumerate(sums):
        acc_hid_two[:, n * 128 : n * 128 + 128] += value
    acc_two[6] += d_out_bias
    acc_two[4] += d_shift
    acc_two[3] += d_gain
    mean_out[0, 0] = spread(by_image(d_shift * gain2) / count_two, 128)
    mean_out[0, 1] = spread(by_image(d_gain * gain2) / count_two, 128)
    keep(gw1_ref, new_gw1)
    keep(gw2_ref, new_gw2)
    d_scale = fold(w2_ref[...].astype(f32) * new_gw2) + out_bias * d_out_bias
    acc_two[5] += d_scale / scale2

    def finish():
        if pairs > 1:
            pack_blocks(range(5))
        else:
            pack_blocks(range(2))

        def filler(number, carry):
            put_block(number, jnp.zeros((HALF, 128), bf16))
            return carry

        lax.fori_loop(USED, slots, filler, 0)

        flat_ref[...] = jnp.zeros(flat_ref.shape, f32)

        def put(at, total, length):
            if at % 128:
                room = jnp.zeros((8, 128), f32)
                if total.shape[1] < length + BS:
                    total = jnp.concatenate([total, room], axis=1)
                total = pltpu.roll(total, BS, 1)
            whole = jnp.sum(total, axis=0, keepdims=True)
            done = -(at % 128)
            row = at // 128
            lane = 0
            while done < length:
                first = max(0, -done)
                last = min(128, length - done)
                flat_ref[row : row + 1, first:last] = whole[:, lane + first : lane + last]
                done += 128
                lane += 128
                row += 1

        at = 3 * C2
        for n in range(3, 6):
            put(at, acc_two[n], C2)
            at += C2
        put(at, acc_hid_two[...], HID2)
        at += HID2
        put(at, acc_two[6], C2)
        at += C2
        for n in range(7):
            put(at, acc_three[n], C3)
            at += C3
        put(at, acc_hid_three[...], HID3)
        at += HID3
        put(at, acc_three[7], C3)

    at_pair(pairs - 1, finish)


def run_main(places, place, buckets, state, goal, vec, weights, strip_count):
    pairs = goal.shape[0]
    slots = places[0].shape[0]
    half = slots // 2 + 1
    if pairs == 1:
        state = held_in(pltpu.VMEM, *state)
    weights = held_in(pltpu.VMEM, *weights)
    _, inv, _, mix, stat = state
    state_shapes = [STATE[1], STATE[3], STATE[4]]
    grad_kind = bf16 if pairs == 1 else f32
    wide_f32 = pltpu.VMEM((AREA, WIDE), f32)
    wide_bf16 = pltpu.VMEM((AREA, WIDE), bf16)
    scratch = [
        pltpu.VMEM((4, AREA + LINE, C2), f32),
        pltpu.VMEM((2, AREA, HID2), f32),
        pltpu.VMEM((4 * AREA, HID2), bf16),
        pltpu.VMEM((4 * AREA, HID2), bf16),
        pltpu.VMEM((4 * AREA, C2), bf16),
        pltpu.VMEM((4 * AREA, C2), bf16),
        pltpu.VMEM((AREA, 9 * C2), bf16),
        pltpu.VMEM((AREA + LINE, 9 * C2), f32),
        pltpu.VMEM((AREA, 128), f32),
        wide_f32,
        pltpu.VMEM((AREA + 2 * LINE, WIDE), f32),
        wide_f32,
        wide_f32,
        wide_f32,
        pltpu.VMEM((AREA, HID3), f32),
        pltpu.VMEM((AREA, HID3), f32),
        pltpu.VMEM((AREA, HID3), bf16),
        pltpu.VMEM((AREA, HID3), bf16),
        wide_bf16,
        wide_bf16,
        wide_bf16,
        pltpu.VMEM((C2, HID2), grad_kind),
        pltpu.VMEM((HID2, C2), grad_kind),
        pltpu.VMEM((9 * C2, WIDE), grad_kind),
        pltpu.VMEM((WIDE, HID3), grad_kind),
        pltpu.VMEM((HID3, WIDE), grad_kind),
        pltpu.VMEM((7, 8, C2), f32),
        pltpu.VMEM((8, HID2), f32),
        pltpu.VMEM((8, 8, WIDE), f32),
        pltpu.VMEM((8, HID3), f32),
    ]
    out_shapes = [(half, HALF, 128), (half, HALF, 128), (VEC_BLOCKS * HALF, 128)]
    make = pltpu.VMEM if pairs == 1 else jax.ShapeDtypeStruct
    return pl.pallas_call(
        functools.partial(main_kernel, pairs, strip_count, slots),
        grid=() if pairs == 1 else (pairs,),
        in_specs=[SMEM] * 4
        + pair_specs(pairs, state_shapes + [goal.shape[1:]], pl.Buffered(1))
        + whole_specs(pairs, [vec.shape])
        + [VMEM_BLOCK] * 5,
        out_specs=pair_specs(pairs, [(AREA, WIDE)] + BACK) + whole_specs(pairs, out_shapes),
        out_shape=pair_arrays(pairs, [(AREA, WIDE)] + BACK, [f32] * 4)
        + [make(shape, kind) for shape, kind in zip(out_shapes, (bf16, bf16, f32))],
        scratch_shapes=scratch,
        compiler_params=pltpu.CompilerParams(
            vmem_limit_bytes=(40 if pairs == 1 else 56) * 1024 * 1024,
            fuse_transposed_lhs_in_matmul=True,
        ),
        name="blocks",
    )(*places, place, buckets, inv, mix, stat, goal, vec, *weights)


def exit_kernel(
    pairs,
    strip_count,
    place_ref,
    bucket_ref,
    x_in,
    inv_in,
    pool_in,
    mix_in,
    stat_in,
    zed_in,
    dx_in,
    mean_in,
    flat_ref,
    vec_ref,
    payload_hbm,
    vector_ref,
    payload_ref,
    image_ref,
    col_ref,
    dx_ref,
    back_ref,
    acc_ref,
    sem,
):
    pair = pl.program_id(0) if pairs > 1 else 0
    x_ref, inv_ref, pool_ref, mix_ref, stat_ref, zed_ref, low_ref, mean_ref = (
        ref.at[0] for ref in (x_in, inv_in, pool_in, mix_in, stat_in, zed_in, dx_in, mean_in)
    )
    bucket_of = bucket_reader(place_ref, bucket_ref, strip_count)
    shape = Geometry(bucket_of, pair)
    count_two = shape.count_two
    gain1, bias1, scale1, gain2 = (vec_ref[n : n + 1] for n in range(4))
    mean1, scaling1, mean2, scaling2 = (stat_ref[n] for n in range(4))
    normal2 = (scaling2, -mean2 * scaling2)
    clear_edges(col_ref)
    nothing = jnp.zeros((8, C2), f32)
    back_gain2 = scaling2 * gain2
    back_mean2 = -scaling2 * mean_ref[0]
    back_normal2 = scaling2 * mean_ref[1]

    if pairs > 1:

        @pl.when(pair == 0)
        def _():
            acc_ref[...] = jnp.zeros(acc_ref.shape, f32)

    def add_up(n, total):
        acc_ref[n] = total if pairs == 1 else acc_ref[n] + total

    def unmix(k, d_scale):
        rows = step_rows(k)
        for pr in range(2):
            weighted = []
            for pc in range(2):
                plane = pr * 2 + pc
                share = inv_ref[plane, rows]
                normal = affine(mix_ref[plane, rows], *normal2)
                back = affine(low_ref[plane, rows], back_gain2, back_mean2)
                back = back - scaled(normal, back_normal2)
                d_mixed = jnp.where(share > 0.0, zed_ref[plane, rows] + back, 0.0)
                dx_ref[plane, rows] = d_mixed
                d_scale = d_scale + fold(pool_ref[plane, rows] * d_mixed)
                weighted.append(scale1 * d_mixed * share)
            put_col_windows(col_ref, pr, k, *weighted)
        return d_scale

    add_up(2, sweep(unmix, nothing))
    normal1 = (spread(scaling1, C2), spread(-mean1 * scaling1, C2))

    def unpool(k, carry):
        d_shift, d_gain = carry
        rows = step_rows(k)
        for pc in range(2):
            windows = row_windows(col_ref, pc, k)
            for pr in range(2):
                plane = pr * 2 + pc
                valid = inv_ref[plane, rows] > 0.0
                d_normal = windows[pr] - scale1 * dx_ref[plane, rows]
                d_normal = jnp.where(valid, d_normal, 0.0)
                back_ref[plane, rows] = d_normal
                normal = affine(x_ref[plane, rows], *normal1)
                d_shift = d_shift + fold(d_normal)
                d_gain = d_gain + fold(d_normal * normal)
        return (d_shift, d_gain)

    d_shift, d_gain = sweep(unpool, (nothing, nothing))
    add_up(1, d_shift)
    add_up(0, d_gain)
    mean_shift = by_image(d_shift * gain1) / count_two
    mean_gain = by_image(d_gain * gain1) / count_two
    back_gain1 = scaling1 * gain1
    back_mean1 = spread(-scaling1 * mean_shift, C2)
    back_normal1 = spread(scaling1 * mean_gain, C2)

    def unnorm(k, carry):
        rows = step_rows(k)
        for plane in range(4):
            normal = affine(x_ref[plane, rows], *normal1)
            back = affine(back_ref[plane, rows], back_gain1, back_mean1)
            back = back - scaled(normal, back_normal1)
            valid = inv_ref[plane, rows] > 0.0
            dx_ref[plane, rows] = jnp.where(valid, dx_ref[plane, rows] + back, 0.0)
        return carry

    sweep(unnorm, 0)

    def give_back(plane, here, spot, there):
        image_ref[spot, there] = dx_ref[plane, here]

    image_ref[...] = jnp.zeros(image_ref.shape, f32)
    each_image(bucket_of, pair, give_back)

    for spot in range(2 * STRIPS):
        target = strip_place(pair, spot, strip_count)
        for within in range(SR):
            rows = slice(within * CW, within * CW + CW)
            payload_ref[target, within] = image_ref[spot, rows].astype(bf16)

    def finish():
        copy = pltpu.make_async_copy(payload_ref, payload_hbm, sem)
        copy.start()
        vector_ref[...] = flat_ref[...]
        for n in range(3):
            vector_ref[n : n + 1] = jnp.sum(acc_ref[n], axis=0, keepdims=True)
        copy.wait()

    if pairs == 1:
        finish()
    else:
        pl.when(pair == pairs - 1)(finish)


def run_exit(place, buckets, state, back, flat, vec, strip_count):
    pairs = strip_count // 8
    payload = (strip_count, SR, CW, C2)
    make = pltpu.VMEM if pairs == 1 else jax.ShapeDtypeStruct
    plane_f32 = pltpu.VMEM((4, AREA, C2), f32)
    arrays = [*state, *back]
    if pairs == 1:
        arrays = held_in(pltpu.VMEM, *arrays)
    return pl.pallas_call(
        functools.partial(exit_kernel, pairs, strip_count),
        grid=() if pairs == 1 else (pairs,),
        in_specs=[SMEM] * 2
        + pair_specs(pairs, STATE + BACK, pl.Buffered(1))
        + whole_specs(pairs, [flat.shape, vec.shape]),
        out_specs=[HBM] + whole_specs(pairs, [flat.shape]),
        out_shape=[pltpu.HBM(payload, bf16), make(flat.shape, f32)],
        scratch_shapes=[
            pltpu.VMEM(payload, bf16),
            pltpu.VMEM((2 * STRIPS, STRIP_ROWS, C2), f32),
            pltpu.VMEM((4, AREA + 2 * LINE, C2), f32),
            plane_f32,
            plane_f32,
            pltpu.VMEM((3, 8, C2), f32),
            pltpu.SemaphoreType.DMA,
        ],
        compiler_params=roomy(8 if pairs == 1 else 40),
        name="exit",
    )(place, buckets, *arrays, flat, vec)


def dense_blocks(values):
    return jnp.concatenate([values[:, :HALF], values[:, HALF:]], axis=2).astype(bf16)


def pack_kernel(master_ref, dense_ref):
    dense_ref[...] = dense_blocks(master_ref[...])


def pack(master):
    owned = master.shape[0]
    return pl.pallas_call(
        pack_kernel,
        out_shape=jax.ShapeDtypeStruct((owned, HALF, 2 * BS), bf16),
        name="pack",
    )(master)


def pack_pieces_kernel(place_ref, master_hbm, pixel_hbm, *refs):
    out_refs, (wide_ref, master_ref, pixel_ref, sem) = refs[:-4], refs[-4:]
    owned = master_ref.shape[0]
    slots = pixel_ref.shape[2]
    copies = [pltpu.make_async_copy(pixel_hbm, pixel_ref, sem.at[0])]
    parts = [(0, owned // 2), (owned // 2, owned - owned // 2)]
    for n, part in enumerate(parts):
        copies.append(
            pltpu.make_async_copy(
                master_hbm.at[pl.ds(*part)], master_ref.at[pl.ds(*part)], sem.at[1 + n]
            )
        )
    for copy in copies:
        copy.start()
    copies[0].wait()

    def widen_row(row, carry):
        start = pl.multiple_of(row * CW * slots, 8)
        values = pixel_ref[row].astype(f32).reshape(CW * slots, C2)
        wide_ref[pl.ds(start, CW * slots)] = values
        return carry

    lax.fori_loop(0, SR, widen_row, 0)
    for k, ref in enumerate(out_refs):
        for other in range(2):
            slot = place_ref[0] ^ (2 * k + other)
            first = other * (ref.shape[0] - STRIP_ROWS)
            strip = wide_ref[pl.ds(slot, STRIP_ROWS, stride=slots)]
            ref[first : first + STRIP_ROWS] = strip.astype(bf16)
    for (first, count), copy in zip(parts, copies[1:]):
        copy.wait()
        dense = dense_blocks(master_ref[first : first + count]).reshape(count * HALF, 2 * BS)
        start = STRIP_ROWS + first * HALF
        for ref in out_refs[:3]:
            ref[start : start + count * HALF] = dense


def pack_pieces(place, master, pixels):
    slots = pixels.shape[2]
    rows = master.shape[0] * HALF
    shapes = [(rows + 2 * STRIP_ROWS, 2 * BS)] * 3 + [(2 * STRIP_ROWS, 2 * BS)]
    return pl.pallas_call(
        pack_pieces_kernel,
        in_specs=[SMEM] + [HBM] * 2,
        out_specs=[VMEM_BLOCK] * 4,
        out_shape=[pltpu.VMEM(shape, bf16) for shape in shapes],
        scratch_shapes=[
            pltpu.VMEM((STRIP_ROWS * slots, C2), f32),
            pltpu.VMEM(master.shape, f32),
            pltpu.VMEM(pixels.shape, bf16),
            pltpu.SemaphoreType.DMA((3,)),
        ],
        compiler_params=roomy(12),
        name="pack",
    )(place, *held_in(pltpu.HBM, master, pixels))


def fold_pair_kernel(near_ref, got_ref, own_ref, *part_refs):
    share = own_ref.shape[0]

    def one(n, carry):
        own_ref[n] = near_ref[n].astype(f32) + got_ref[n].astype(f32)
        for k, ref in enumerate(part_refs):
            here = (k + 1) * share + n
            ref[n] = near_ref[here] + got_ref[here]
        return carry

    lax.fori_loop(0, share, one, 0, unroll=4)


def fold_pair(near, got, groups):
    shape = ((near.shape[0] - 1) // groups,) + near.shape[1:]
    return pl.pallas_call(
        fold_pair_kernel,
        in_specs=[VMEM_BLOCK] * 2,
        out_specs=[VMEM_BLOCK] * groups,
        out_shape=[pltpu.VMEM(shape, f32)] + [pltpu.VMEM(shape, bf16)] * (groups - 1),
        compiler_params=roomy(4),
        name="fold_pair",
    )(*held_in(pltpu.VMEM, near, got))


def fold_tile_kernel(pieces, spot_ref, *refs):
    piece_refs, refs = refs[:pieces], refs[pieces:]
    vector_refs, refs = refs[:pieces], refs[pieces:]
    out_refs, sum_ref = refs[:-1], refs[-1]
    groups = len(out_refs)
    share = out_refs[0].shape[0]
    owned = piece_refs[0].shape[0]
    total = vector_refs[0][...]
    for ref in vector_refs[1:]:
        total = total + ref[...]
    for n in range(sum_ref.shape[0]):
        sum_ref[n] = jnp.zeros((HALF, 128), f32)
    for n in range(VEC_BLOCKS):
        sum_ref[n] = total[n * HALF : (n + 1) * HALF]

    def one(n, carry):
        for k, out_ref in enumerate(out_refs):
            number = lax.rem(spot_ref[0] + k, groups) * share + n
            block = jnp.minimum(number, owned - 1)
            total = piece_refs[0][block].astype(f32)
            for ref in piece_refs[1:]:
                total = total + ref[block].astype(f32)
            rest = sum_ref[jnp.maximum(number - owned, 0)]
            out_ref[n] = jnp.where(number < owned, total, rest).astype(out_ref.dtype)
        return carry

    lax.fori_loop(0, share, one, 0, unroll=share <= 16)


def fold_tile(spot, pieces, vectors, extra, groups):
    shape = ((pieces[0].shape[0] + extra) // groups,) + pieces[0].shape[1:]
    return pl.pallas_call(
        functools.partial(fold_tile_kernel, len(pieces)),
        in_specs=[SMEM] + [VMEM_BLOCK] * (len(pieces) + len(vectors)),
        out_specs=[VMEM_BLOCK] * groups,
        out_shape=[pltpu.VMEM(shape, f32)] + [pltpu.VMEM(shape, bf16)] * (groups - 1),
        scratch_shapes=[pltpu.VMEM((extra, HALF, 128), f32)],
        compiler_params=roomy(8),
        name="fold_tile",
    )(spot, *held_in(pltpu.VMEM, *pieces, *vectors))


def fold_batch_kernel(owned, vector_weight, spot_ref, *refs):
    part_refs, (total_ref, norm_ref) = refs[:-2], refs[-2:]
    share = total_ref.shape[0]
    square = jnp.zeros((8, 128), f32)
    for n in range(share):
        total = part_refs[0][n].astype(f32)
        for ref in part_refs[1:]:
            total = total + ref[n].astype(f32)
        total_ref[n] = total.astype(bf16)
        weight = jnp.where(spot_ref[0] * share + n < owned, 1.0, vector_weight)
        square = square + weight * fold(total * total)
    square = jnp.sum(jnp.sum(square, axis=1, keepdims=True), axis=0, keepdims=True)
    norm_ref[...] = jnp.broadcast_to(square[None], norm_ref.shape)


def fold_batch(spot, parts, owned, tile_count):
    count = tile_count * len(parts)
    return pl.pallas_call(
        functools.partial(fold_batch_kernel, owned, 1.0 / tile_count),
        in_specs=[SMEM] + [VMEM_BLOCK] * len(parts),
        out_specs=[VMEM_BLOCK] * 2,
        out_shape=[pltpu.VMEM(parts[0].shape, bf16), pltpu.VMEM((count, 1, 128), f32)],
        name="fold_batch",
    )(spot, *held_in(pltpu.VMEM, *parts))


def update_kernel(owned, groups, spot_ref, norm_ref, *refs):
    quarters, refs = refs[:groups], refs[groups:]
    stat_hbm, out_hbm, (vector_ref, clip_ref), refs = refs[:5], refs[5:10], refs[10:12], refs[12:]
    stat_refs, out_refs, (in_sem, out_sem) = refs[:5], refs[5:10], refs[10:]
    master_ref, left_stat_ref, right_stat_ref, left_root_ref, right_root_ref = stat_refs
    grad_ref, left_ref, right_ref, new_ref, copy_ref = out_refs
    share = quarters[0].shape[0]
    spans = spans_of(owned)

    def copies_of(sources, targets, sems):
        return [
            [
                pltpu.make_async_copy(
                    source.at[pl.ds(*span)], target.at[pl.ds(*span)], sems.at[5 * n + k]
                )
                for k, (source, target) in enumerate(zip(sources, targets))
            ]
            for n, span in enumerate(spans)
        ]

    copies_in = copies_of(stat_hbm, stat_refs, in_sem)
    copies_out = copies_of(out_refs, out_hbm, out_sem)
    for copies in copies_in:
        for copy in copies:
            copy.start()
    norm = jnp.sqrt(jnp.sum(norm_ref[...], axis=0))
    factor = jnp.minimum(1.0, clip_limit / norm)
    left_half = lax.broadcasted_iota(jnp.int32, (HALF, 128), 1) < BS

    def summed(number):
        source = number // share
        local = number - source * share
        turn = lax.rem(spot_ref[0] - source + groups, groups)
        value = quarters[0][local].astype(f32)
        for k in range(1, groups):
            value = jnp.where(turn == k, quarters[k][local].astype(f32), value)
        return value * factor

    def side_by_side(first, count):
        sides = []
        for n in range(first, first + count, 2):
            dense = summed(n)
            turned = pltpu.roll(dense, BS, 1)
            if n + 1 < first + count:
                second = summed(n + 1)
                top = jnp.where(left_half, dense, pltpu.roll(second, BS, 1))
                low = jnp.where(left_half, turned, second)
                side = jnp.concatenate([top, low], axis=0)
                grad_ref[n + 1] = pltpu.roll(side, BS, 1)[:, :BS]
            else:
                side = jnp.concatenate([dense, turned], axis=0)[:, :BS]
            grad_ref[n] = side[:, :BS]
            sides.append(side.astype(bf16))
        return jnp.concatenate(sides, axis=1)

    def diagonal_of(count):
        order = (count * BS, count * BS)
        return lax.broadcasted_iota(jnp.int32, order, 0) // BS == (
            lax.broadcasted_iota(jnp.int32, order, 1) // BS
        )

    clip_ref[...] = norm
    for n in range(vector_ref.shape[0]):
        vector_ref[n] = summed(owned + n)
    for (first, length), arriving, leaving in zip(spans, copies_in, copies_out):
        parts = [(n, min(4, first + length - n)) for n in range(first, first + length, 4)]
        wides = [side_by_side(*part) for part in parts]
        tall = [
            jnp.where(diagonal_of(count), jnp.concatenate([wide] * count, axis=0), 0.0)
            for (_, count), wide in zip(parts, wides)
        ]
        lefts = [product_nt(one, wide) for one, wide in zip(tall, wides)]
        rights = [product_tn(wide, wide) for wide in wides]
        for copy in arriving:
            copy.wait()
        stepped = []
        for (start, count), wide in zip(parts, wides):
            roots = left_root_ref[pl.ds(start, count)].reshape(count * BS, BS).astype(bf16)
            stepped.append(product(roots, wide))
        for (start, count), left, right in zip(parts, lefts, rights):
            here = pl.ds(start, count)
            left_ref[here] = 0.5 * left_stat_ref[here] + 0.5 * left.reshape(count, BS, BS)
            for n in range(count):
                at = n // 2 * 128
                block = right[n * BS : n * BS + BS, at : min(at + 128, count * BS)]
                if n % 2:
                    block = pltpu.roll(block, BS, 1)
                right_ref[start + n] = 0.5 * right_stat_ref[start + n] + 0.5 * block[:, :BS]
        for (start, count), value in zip(parts, stepped):
            here = pl.ds(start, count)
            value = jnp.where(diagonal_of(count), value, 0.0).astype(bf16)
            roots = right_root_ref[here].reshape(count * BS, BS).astype(bf16)
            value = product(value, roots).reshape(count, BS, BS)
            new = master_ref[here] - rate_matrix * value
            new_ref[here] = new
            copy_ref[here] = new.astype(bf16)
        for copy in leaving:
            copy.start()
    for leaving in copies_out:
        for copy in leaving:
            copy.wait()


def spans_of(owned):
    spans = []
    first = 0
    while first < owned:
        length = min(8 if first == 0 else 12, owned - first)
        spans.append((first, length))
        first += length
    return spans


def update(spot, norm, quarters, extra, *stats):
    shape = stats[0].shape
    groups = len(quarters)
    types = [f32] * 4 + [bf16]
    steps = len(spans_of(shape[0]))
    return pl.pallas_call(
        functools.partial(update_kernel, shape[0], groups),
        in_specs=[SMEM] + [VMEM_BLOCK] * (groups + 1) + [HBM] * 5,
        out_specs=[HBM] * 5 + [VMEM_BLOCK] * 2,
        out_shape=[pltpu.HBM(shape, kind) for kind in types]
        + [
            pltpu.VMEM((extra, HALF, 128), f32),
            pltpu.VMEM((1, 128), f32),
        ],
        scratch_shapes=[pltpu.VMEM(shape, f32)] * 5
        + [pltpu.VMEM(shape, kind) for kind in types]
        + [
            pltpu.SemaphoreType.DMA((5 * steps,)),
            pltpu.SemaphoreType.DMA((5 * steps,)),
        ],
        compiler_params=roomy(20),
        name="update",
    )(spot, *held_in(pltpu.VMEM, norm, *quarters), *held_in(pltpu.HBM, *stats))


def share_out(pieces, axis):
    return lax.all_to_all(pieces, axis, split_axis=0, concat_axis=0, tiled=True)


def swap(piece, distance):
    count = lax.axis_size("tile")
    return lax.ppermute(piece, "tile", [(i, i ^ distance) for i in range(count)])


def on_device(
    pixels,
    buckets,
    slot_owner_table,
    out_grad,
    master,
    left_stat,
    right_stat,
    left_root,
    right_root,
    vectors,
    moment,
):
    tile_count = lax.axis_size("tile")
    tile_place = lax.axis_index("tile")
    slot_count = pixels.shape[2]
    group_count = tile_count // STRIPS
    pairs = group_count // 2
    owned = master.shape[0]
    slots = owned * tile_count
    batch_count = lax.axis_size("batch")
    spot = lax.axis_index("batch").astype(jnp.int32).reshape(1)
    extra = extra_of(owned, batch_count)
    place = tile_place.astype(jnp.int32).reshape(1)
    paired = tile_count == 8
    numbers = jnp.arange(slots, dtype=jnp.int32)
    slot_of = jnp.sum(
        jnp.where(slot_owner_table[None, :] == numbers[:, None], numbers[None, :], 0), axis=1
    )
    if paired:
        owner = slot_of // owned
        apart = owner ^ tile_place
        apart = (apart & 1) * (tile_count // 2) + (apart >> 1)
        slot_of = slot_of + owned * (apart - owner)
    half = slots // 2
    near_place = jnp.where(slot_of < half, slot_of, half)
    far_place = jnp.where(slot_of < half, half, slot_of - half)
    vec = vectors.reshape(-1, 128)
    turned = lax.dynamic_index_in_dim(
        buckets.reshape(group_count, slot_count), tile_place, 1, keepdims=False
    ) >= 2
    flips = turned.reshape(-1, 1, 1, 1)
    goal = out_grad.reshape(2 * pairs, H3, W3, C3)
    goal = jnp.where(flips, goal.transpose(0, 2, 1, 3), goal)[:, :LINES]
    goal = goal.reshape(pairs, 2, LINES, W3, C3).transpose(0, 2, 3, 1, 4)
    goal = goal.reshape(pairs, LINES, 2 * W3, C3)
    goal = jnp.pad(goal, ((0, 0), (0, 0), (0, LINE - 2 * W3), (0, WIDE - C3)))
    goal = goal.reshape(pairs, AREA, WIDE)

    if paired:
        own, for_x, for_y, for_both = pack_pieces(
            place, master, pixels[0, 0].transpose(1, 2, 0, 3)
        )
        goal, vec, slot_of, near_place, far_place, own = lax.optimization_barrier(
            (goal, vec, slot_of, near_place, far_place, own)
        )
        from_x, from_y, strips_both = swap(for_x, 2), swap(for_y, 4), swap(for_both, 6)
        near_half = (owned + 1) // 2
        middle = STRIP_ROWS + near_half * HALF
        first_half = swap(from_x[STRIP_ROWS:middle], 4)
        second_half = swap(from_y[middle : STRIP_ROWS + owned * HALF], 2)
        mine = [own, from_x, from_y, strips_both]
        theirs = [swap(piece, 1) for piece in mine]
        state = run_entry(place, buckets, mine + theirs, vec, tile_count)
        *state, first_half = lax.optimization_barrier((*state, first_half))
        pieces = mine[:3] + [first_half, second_half]
        pieces += theirs[:3] + [swap(first_half, 1), swap(second_half, 1)]
        spans = [(STRIP_ROWS, owned)] * 3 + [(0, near_half), (0, owned - near_half)]
        spans = spans * 2
    else:
        pieces = [lax.all_gather(pack(master), "tile", axis=0, tiled=True).reshape(-1, 2 * BS)]
        spans = [(0, slots)]
        strips = share_out(pixels.reshape(tile_count, STRIP, C2), "tile")
        strips = [jnp.pad(strips, ((0, 0), (0, STRIP_ROWS - STRIP), (0, 0)))]
        state = run_entry(place, buckets, strips, vec, tile_count)

    weights = run_unpack(slot_of, pieces, spans)
    result, *back, near, far, flat = run_main(
        (near_place, far_place),
        place,
        buckets,
        state,
        goal,
        vec,
        weights,
        tile_count,
    )
    pixel_back, vector = run_exit(place, buckets, state, back, flat, vec, tile_count)
    if paired:
        own, *parts = fold_pair(near, swap(far, 1), tile_count // 2)
        pieces = [own] + [swap(part, 2 * k + 2) for k, part in enumerate(parts)]
        vector, _ = lax.optimization_barrier((vector, parts[0]))
        vector = vector + swap(vector, 1)
        vectors_in = [vector] + [swap(vector, 2 * k) for k in range(1, tile_count // 2)]
    else:
        outgoing = jnp.concatenate([near[:half], far[:half]], axis=0)
        pieces = list(share_out(outgoing.reshape(tile_count, owned, HALF, 128), "tile"))
        vectors_in = list(lax.all_gather(vector, "tile"))
    result, pieces[1] = lax.optimization_barrier((result, pieces[1]))
    result = result.reshape(pairs, LINES, LINE, WIDE)[:, :, : 2 * W3, :C3]
    result = result.reshape(pairs, LINES, W3, 2, C3).transpose(0, 3, 1, 2, 4)
    result = result.reshape(2 * pairs, LINES, W3, C3)
    result = jnp.pad(result, ((0, 0), (0, H3 - LINES), (0, 0), (0, 0)))
    result = jnp.where(flips, result.transpose(0, 2, 1, 3), result)
    result = result.reshape(out_grad.shape)
    result = with_layout_constraint(result, Layout(major_to_minor=(0, 1, 2, 4, 5, 3, 6)))
    result, vectors_in[0] = lax.optimization_barrier((result, vectors_in[0]))
    own, *parts = fold_tile(spot, pieces, vectors_in, extra, batch_count)
    pixel_back, parts[0] = lax.optimization_barrier((pixel_back, parts[0]))
    returned = share_out(pixel_back, "tile")
    parts = [
        lax.ppermute(part, "batch", [(i, (i + k + 1) % batch_count) for i in range(batch_count)])
        for k, part in enumerate(parts)
    ]
    quarter, norm = fold_batch(spot, [own] + parts, owned, tile_count)
    returned, norm = lax.optimization_barrier((returned, norm))
    norm = share_out(norm, ("batch", "tile"))
    returned = returned.astype(f32).reshape(pixels.shape)
    returned = with_layout_constraint(returned, Layout(major_to_minor=(0, 1, 3, 4, 2, 5)))
    returned, quarter = lax.optimization_barrier((returned, quarter))
    quarters = [quarter] + [
        lax.ppermute(quarter, "batch", [(i, (i + k) % batch_count) for i in range(batch_count)])
        for k in range(1, batch_count)
    ]
    block_grad, left_new, right_new, master_new, weight_copy, whole_vector, clip = update(
        spot, norm, quarters, extra, master, left_stat, right_stat, left_root, right_root
    )
    clip_norm = clip[0, 0]
    share = vectors.shape[0] // tile_count
    whole_vector = whole_vector.reshape(-1)
    vec_grad = lax.dynamic_slice_in_dim(whole_vector, tile_place * share, share, 0)
    vec_moment = moment + vec_grad * vec_grad
    own_vectors = lax.dynamic_slice_in_dim(vectors, tile_place * share, share, 0)
    vec_new = own_vectors - rate_vector * vec_grad / (jnp.sqrt(vec_moment) + eps_adagrad)
    return (
        result,
        returned,
        clip_norm,
        block_grad,
        left_new,
        right_new,
        master_new,
        weight_copy,
        vec_grad,
        vec_moment,
        vec_new,
    )


def solution(mesh):
    placed = (
        P("batch", "tile", None, None, None, None),
        P("batch"),
        P(),
        P("batch", "tile", None, None, None, None, None),
        P("tile", None, None),
        P("tile", None, None),
        P("tile", None, None),
        P("tile", None, None),
        P("tile", None, None),
        P(),
        P("tile"),
    )
    return jax.shard_map(
        on_device,
        mesh=mesh,
        in_specs=placed,
        out_specs=(
            P("batch", "tile", None, None, None, None, None),
            P("batch", "tile", None, None, None, None),
            P(),
            P("tile", None, None),
            P("tile", None, None),
            P("tile", None, None),
            P("tile", None, None),
            P("tile", None, None),
            P("tile"),
            P("tile"),
            P("tile"),
        ),
        check_vma=False,
    )
```

```python
import functools

import jax
import jax.numpy as jnp
from jax import lax
from jax.experimental import pallas as pl
from jax.experimental.layout import Layout, with_layout_constraint
from jax.experimental.pallas import tpu as pltpu
from jax.sharding import PartitionSpec as P

C2 = 128
HID2 = 512
C3 = 320
HID3 = 1280
CH = 36
CW = 36
STRIPS = 4
BS = 64
SR = CH // STRIPS
H3 = CH // 2
W3 = CW // 2
LONG = 7 * CH // 9
LINES = LONG // 2
WIDE = 384
LINE = 40
AREA = LINES * LINE
STEP = 2 * LINE
STEPS = AREA // STEP
HALF = BS // 2
STRIP = SR * CW
STRIP_ROWS = STRIP + -STRIP % 16

eps_norm = 1e-05
clip_limit = 1.0
rate_matrix = 0.3
rate_vector = 0.3
eps_adagrad = 1e-08
f32 = jnp.float32
bf16 = jnp.bfloat16

SHAPES = [(C2, HID2), (HID2, C2), (9 * C2, C3), (C3, HID3), (HID3, C3)]
USED = sum(rows // BS * (cols // BS) for rows, cols in SHAPES)
VEC_ROWS = (6 * C2 + HID2 + C2 + C3 + 6 * C3 + HID3 + C3) // 128


VEC_BLOCKS = -(-VEC_ROWS // HALF)


def extra_of(owned, groups):
    return VEC_BLOCKS + -(owned + VEC_BLOCKS) % groups


def product(left, right):
    return jnp.dot(left, right, preferred_element_type=f32)


def product_nt(left, right):
    return lax.dot_general(left, right, (((1,), (1,)), ((), ())), preferred_element_type=f32)


def product_tn(left, right):
    return lax.dot_general(left, right, (((0,), (0,)), ((), ())), preferred_element_type=f32)


def gelu_pair(values):
    bell = jnp.exp2(values * values * (-0.5 * 1.4426950408889634))
    step = pl.reciprocal(1.0 + (0.3275911 * 0.7071067811865476) * jnp.abs(values), approx=True)
    tail = step * (
        0.5 * 0.254829592
        + step
        * (
            0.5 * -0.284496736
            + step
            * (0.5 * 1.421413741 + step * (0.5 * -1.453152027 + step * (0.5 * 1.061405429)))
        )
    )
    tail = tail * bell
    share = jnp.where(values >= 0.0, 1.0 - tail, tail)
    return (values * share, share + values * (bell * 0.3989422804014327))


def fold(values):
    chans = values.shape[-1]
    return jnp.sum(values.reshape(-1, 8, chans), axis=0)


def by_image(total):
    total = total + pltpu.roll(total, 4, 0)
    total = total + pltpu.roll(total, 2, 0)
    return jnp.sum(total, axis=1, keepdims=True)


def line(pattern):
    return jnp.concatenate([pattern] * (LINE // 8), axis=0)


def spread(pattern, chans):
    return jnp.broadcast_to(pattern, (8, chans))


def affine(values, factor, shift):
    tiles = values.reshape(-1, 8, values.shape[-1])
    return (tiles * factor + shift).reshape(values.shape)


def scaled(values, factor):
    tiles = values.reshape(-1, 8, values.shape[-1])
    return (tiles * factor).reshape(values.shape)


def from_left(values):
    return pltpu.roll(values, 2, 0)


def from_right(values):
    return pltpu.roll(values, values.shape[0] - 2, 0)


def rounded(values):
    return values.astype(bf16).astype(f32)


def widen(values):
    return jnp.concatenate([values] * (WIDE // 128), axis=-1)


def norm_terms(total, square, count):
    mean = by_image(total) / count
    scaling = lax.rsqrt(by_image(square) / count - mean * mean + eps_norm)
    return (mean, scaling)


def sweep(visit, start):
    return lax.fori_loop(0, STEPS, visit, start, unroll=True)


def step_rows(k, lines=0):
    start = k * STEP + lines * LINE
    return pl.ds(start if isinstance(k, int) else pl.multiple_of(start, LINE), STEP)


def held_in(space, *arrays):
    return [pltpu.with_memory_space_constraint(array, space) for array in arrays]


VMEM_BLOCK = pl.BlockSpec(memory_space=pltpu.VMEM)
HBM = pl.BlockSpec(memory_space=pltpu.HBM)
SMEM = pl.BlockSpec(memory_space=pltpu.SMEM)


def roomy(mebibytes):
    return pltpu.CompilerParams(vmem_limit_bytes=mebibytes * 1024 * 1024)


def image_shape(bucket_of, pair, image):
    bucket = bucket_of(2 * pair + image)
    plain = jnp.where(bucket == 0, 5 * CH // 9, 7 * CH // 9)
    across = jnp.where(bucket == 0, CW, 7 * CW // 9)
    turned = (bucket >= 2).astype(jnp.int32)
    return (
        jnp.where(turned > 0, 5 * CW // 9, plain),
        jnp.where(turned > 0, CH, across),
        turned,
    )


def bucket_reader(place_ref, bucket_ref, strip_count):
    return lambda group: bucket_ref[group * strip_count + place_ref[0]]


class Geometry:
    def __init__(self, bucket_of, pair):
        parity = lax.broadcasted_iota(jnp.int32, (8, 128), 0) % 2
        even, odd = (image_shape(bucket_of, pair, image) for image in range(2))
        high, broad, turned = (jnp.where(parity == 0, a, b) for a, b in zip(even, odd))
        self.high = high
        self.count_two = (high * broad * C2).astype(f32)[:, :1]
        self.high3 = (high + 1) // 2
        broad3 = (broad + 1) // 2
        self.count_three = (self.high3 * broad3 * C3).astype(f32)[:, :1]
        place = lax.broadcasted_iota(jnp.int32, (LINE, 128), 0) // 2
        inside = lax.broadcasted_iota(jnp.int32, (LINE, 128), 0) < 2 * W3
        self.reach = []
        self.col_share = []
        for pc in range(2):
            column = 2 * place + pc
            self.reach.append(jnp.where(inside & (column < line(broad)), line(high), 0))
            edge = (column == 0) | (column == line(broad) - 1)
            self.col_share.append(jnp.where(edge, 0.5, 1.0 / 3.0))
        self.reach3 = jnp.where(inside & (place < line(broad3)), line(self.high3), 0)
        edge3 = (place == 0) | (place == line(broad3) - 1)
        self.col_share3 = jnp.where(edge3, 0.5, 1.0 / 3.0)
        self.flipped = jnp.concatenate([turned] * (STEP // 8), axis=0) > 0

    def share(self, plane, k):
        pr, pc = plane // 2, plane % 2
        return self.lines(4 * k + pr, 2, self.reach[pc], self.col_share[pc], self.high)

    def share3(self, k):
        return self.lines(2 * k, 1, self.reach3, self.col_share3, self.high3)

    def lines(self, row, stride, reach, col_share, height):
        parts = []
        for n in range(2):
            here = row + stride * n
            row_share = jnp.where((here == 0) | (here == height - 1), 0.5, 1.0 / 3.0)
            parts.append(jnp.where(here < reach, line(row_share) * col_share, 0.0))
        return jnp.concatenate(parts, axis=0)


def strip_place(pair, spot, strip_count):
    return lax.rem(pair * 8 + strip_count - 2 + spot, strip_count)


def each_image(bucket_of, pair, visit):
    for image in range(2):
        way = image_shape(bucket_of, pair, image)[2]

        @pl.when(way == 0)
        def _():
            def one(r, carry):
                for plane in range(4):
                    row = 2 * r + plane // 2
                    strip = row // SR
                    there = pl.ds((row - strip * SR) * CW + plane % 2, W3, stride=2)
                    here = pl.ds(r * LINE + image, W3, stride=2)
                    visit(plane, here, image * STRIPS + strip, there)
                return carry

            lax.fori_loop(0, LINES, one, 0)

        @pl.when(way == 1)
        def _():
            def one(r, carry):
                for plane in range(4):
                    for strip in range(STRIPS):
                        first = (plane % 2 + strip * SR) % 2
                        count = (SR - first + 1) // 2
                        done = (strip * SR + first) // 2
                        column = 2 * r + plane // 2
                        there = pl.ds(first * CW + column, count, stride=2 * CW)
                        here = pl.ds(r * LINE + image + 2 * done, count, stride=2)
                        visit(plane, here, image * STRIPS + strip, there)
                return carry

            lax.fori_loop(0, LINES, one, 0)


def row_windows(col_ref, pc, k):
    both = col_ref[pc, step_rows(k, 1)] + col_ref[2 + pc, step_rows(k, 1)]
    return (both + col_ref[2 + pc, step_rows(k)], both + col_ref[pc, step_rows(k, 2)])


def put_col_windows(col_ref, pr, k, even, odd):
    both = even + odd
    col_ref[pr * 2, step_rows(k, 1)] = both + from_left(odd)
    col_ref[pr * 2 + 1, step_rows(k, 1)] = both + from_right(even)


def clear_edges(col_ref):
    zero_line = jnp.zeros((LINE, C2), f32)
    for plane in range(4):
        col_ref[plane, 0:LINE] = zero_line
        col_ref[plane, AREA + LINE : AREA + 2 * LINE] = zero_line


def entry_kernel(pairs, strip_count, piece_count, place_ref, bucket_ref, vec_ref, *refs):
    piece_refs, refs = refs[:piece_count], refs[piece_count:]
    x_out, inv_out, pool_out, mix_out, stat_out, image_ref, col_ref = refs
    pair = pl.program_id(0) if pairs > 1 else 0
    x_ref, inv_ref, pool_ref, mix_ref = (ref.at[0] for ref in (x_out, inv_out, pool_out, mix_out))
    bucket_of = bucket_reader(place_ref, bucket_ref, strip_count)
    shape = Geometry(bucket_of, pair)
    gain1, bias1, scale1 = (vec_ref[n : n + 1] for n in range(3))
    clear_edges(col_ref)
    if piece_count > 1:
        half = piece_count // 2
        for n, ref in enumerate(piece_refs):
            source = place_ref[0] ^ (n // half + 2 * (n % half))
            spot = lax.rem(source + 2, 2 * STRIPS)
            first = 0 if n < half else ref.shape[0] - STRIP_ROWS
            image_ref[spot] = ref[first : first + STRIP_ROWS].astype(f32)
    else:
        for spot in range(2 * STRIPS):
            source = strip_place(pair, spot, strip_count)
            image_ref[spot] = piece_refs[0][source].astype(f32)

    def take_in(plane, here, spot, there):
        x_ref[plane, here] = image_ref[spot, there]

    each_image(bucket_of, pair, take_in)

    def arrange(k, carry):
        total, square = carry
        rows = step_rows(k)
        for plane in range(4):
            share = shape.share(plane, k)
            inv_ref[plane, rows] = share
            values = jnp.where(share > 0.0, x_ref[plane, rows], 0.0)
            x_ref[plane, rows] = values
            total = total + fold(values)
            square = square + fold(values * values)
        return (total, square)

    nothing = jnp.zeros((8, C2), f32)
    total, square = sweep(arrange, (nothing, nothing))
    mean1, scaling1 = norm_terms(total, square, shape.count_two)
    factor1 = scaling1 * gain1
    shift1 = bias1 - mean1 * scaling1 * gain1

    def window_cols(k, carry):
        rows = step_rows(k)
        for pr in range(2):
            masked = []
            for pc in range(2):
                plane = pr * 2 + pc
                normal = rounded(affine(x_ref[plane, rows], factor1, shift1))
                masked.append(jnp.where(inv_ref[plane, rows] > 0.0, normal, 0.0))
            put_col_windows(col_ref, pr, k, *masked)
        return carry

    sweep(window_cols, 0)

    def mix(k, carry):
        total, square = carry
        rows = step_rows(k)
        for pc in range(2):
            windows = row_windows(col_ref, pc, k)
            for pr in range(2):
                plane = pr * 2 + pc
                values = x_ref[plane, rows]
                share = inv_ref[plane, rows]
                pooled = windows[pr] * share - rounded(affine(values, factor1, shift1))
                pooled = jnp.where(share > 0.0, pooled, 0.0)
                mixed = values + scale1 * pooled
                pool_ref[plane, rows] = pooled
                mix_ref[plane, rows] = mixed
                total = total + fold(mixed)
                square = square + fold(mixed * mixed)
        return (total, square)

    total, square = sweep(mix, (nothing, nothing))
    mean2, scaling2 = norm_terms(total, square, shape.count_two)
    for n, value in enumerate((mean1, scaling1, mean2, scaling2)):
        stat_out[0, n] = spread(value, 128)


def pair_specs(pairs, shapes, mode=None):
    if pairs == 1:
        return [VMEM_BLOCK] * len(shapes)
    return [
        pl.BlockSpec(
            (1,) + shape, lambda t, rank=len(shape): (t,) + (0,) * rank, pipeline_mode=mode
        )
        for shape in shapes
    ]


def whole_specs(pairs, shapes):
    if pairs == 1:
        return [VMEM_BLOCK] * len(shapes)
    return [
        pl.BlockSpec(
            shape,
            lambda t, rank=len(shape): (0,) * rank,
            pipeline_mode=pl.Buffered(1),
        )
        for shape in shapes
    ]


def pair_arrays(pairs, shapes, kinds):
    make = pltpu.VMEM if pairs == 1 else jax.ShapeDtypeStruct
    return [make((pairs,) + shape, kind) for shape, kind in zip(shapes, kinds)]


STATE = [(4, AREA, C2)] * 4 + [(4, 8, 128)]
BACK = [(4, AREA, C2)] * 2 + [(2, 8, 128)]


def run_entry(place, buckets, pieces, vec, strip_count):
    pairs = strip_count // 8
    if pairs == 1:
        pieces = held_in(pltpu.VMEM, *pieces)
    return pl.pallas_call(
        functools.partial(entry_kernel, pairs, strip_count, len(pieces)),
        grid=() if pairs == 1 else (pairs,),
        in_specs=[SMEM] * 2 + whole_specs(pairs, [array.shape for array in (vec, *pieces)]),
        out_specs=pair_specs(pairs, STATE),
        out_shape=pair_arrays(pairs, STATE, [f32] * 5),
        scratch_shapes=[
            pltpu.VMEM((2 * STRIPS, STRIP_ROWS, C2), f32),
            pltpu.VMEM((4, AREA + 2 * LINE, C2), f32),
        ],
        compiler_params=roomy(6 if pairs == 1 else 40),
        name="entry",
    )(place, buckets, vec, *pieces)


WEIGHTS = [(C2, HID2), (HID2, C2), (9 * C2, WIDE), (WIDE, HID3), (HID3, WIDE)]


def unpack_kernel(spans, slot_ref, *refs):
    piece_refs, refs = refs[: len(spans)], refs[len(spans) :]
    weights, gathered_ref = refs[:-1], refs[-1]
    done = 0
    for ref, (first, count) in zip(piece_refs, spans):
        blocks = ref[first : first + count * HALF].reshape(count, HALF, 128)
        gathered_ref[done : done + count] = blocks
        done += count
    left_half = lax.broadcasted_iota(jnp.int32, (HALF, 128), 1) < BS
    offset = 0
    for (rows, cols), ref in zip(SHAPES, weights):
        wide = cols // BS
        for rb in range(rows // BS):
            for cb in range(0, wide, 2):
                number = offset + rb * wide + cb
                first = gathered_ref[slot_ref[number]]
                turned = pltpu.roll(first, BS, 1)
                if cb + 1 < wide:
                    second = gathered_ref[slot_ref[number + 1]]
                    top = jnp.where(left_half, first, pltpu.roll(second, BS, 1))
                    low = jnp.where(left_half, turned, second)
                else:
                    top = jnp.where(left_half, first, 0.0)
                    low = jnp.where(left_half, turned, 0.0)
                place = slice(cb * BS, cb * BS + 128)
                ref[rb * BS : rb * BS + HALF, place] = top
                ref[rb * BS + HALF : rb * BS + BS, place] = low
        offset += rows // BS * wide
    weights[3][C3:, :] = jnp.zeros((WIDE - C3, HID3), bf16)


def run_unpack(slot_of, pieces, spans):
    slots = slot_of.shape[0]
    return pl.pallas_call(
        functools.partial(unpack_kernel, spans),
        in_specs=[SMEM] + [VMEM_BLOCK] * len(pieces),
        out_specs=[VMEM_BLOCK] * 5,
        out_shape=[pltpu.VMEM(shape, bf16) for shape in WEIGHTS],
        scratch_shapes=[pltpu.VMEM((slots, HALF, 128), bf16)],
        compiler_params=roomy(6),
        name="unpack",
    )(slot_of, *held_in(pltpu.VMEM, *pieces))


def main_kernel(
    pairs,
    strip_count,
    slots,
    near_place,
    far_place,
    place_ref,
    bucket_ref,
    inv_in,
    mix_in,
    stat_in,
    goal_ref,
    vec_ref,
    w1_ref,
    w2_ref,
    we_ref,
    w3_ref,
    w4_ref,
    result_ref,
    zed_out,
    dx_out,
    mean_out,
    near_ref,
    far_ref,
    flat_ref,
    zed_ref,
    hid_ref,
    u_ref,
    g_ref,
    h_ref,
    dy_ref,
    patch_ref,
    dpatch_ref,
    inv3_ref,
    e_ref,
    col3_ref,
    pool3_ref,
    mix3_ref,
    dx3_ref,
    hid3_ref,
    dhid3_ref,
    u3_ref,
    g3_ref,
    h3_ref,
    dy3_ref,
    dpre_ref,
    gw1_ref,
    gw2_ref,
    gwe_ref,
    gw3_ref,
    gw4_ref,
    acc_two,
    acc_hid_two,
    acc_three,
    acc_hid_three,
):
    pair = pl.program_id(0) if pairs > 1 else 0
    grads = [gw1_ref, gw2_ref, gwe_ref, gw3_ref, gw4_ref]
    inv_ref, mix_ref, stat_ref = (ref.at[0] for ref in (inv_in, mix_in, stat_in))
    back_ref, dx_ref = zed_out.at[0], dx_out.at[0]
    left_half = lax.broadcasted_iota(jnp.int32, (HALF, 128), 1) < BS

    def at_pair(number, act):
        if pairs == 1:
            act()
        else:
            pl.when(pair == number)(act)

    def begin():
        acc_two[...] = jnp.zeros(acc_two.shape, f32)
        acc_hid_two[...] = jnp.zeros(acc_hid_two.shape, f32)
        acc_three[...] = jnp.zeros(acc_three.shape, f32)
        acc_hid_three[...] = jnp.zeros(acc_hid_three.shape, f32)

    at_pair(0, begin)
    shape = Geometry(bucket_reader(place_ref, bucket_ref, strip_count), pair)
    count_two, count_three, flipped = shape.count_two, shape.count_three, shape.flipped
    nothing = jnp.zeros((8, C2), f32)
    nothing3 = jnp.zeros((8, WIDE), f32)

    def vector_row(at, length):
        first, shift = at // 128, at % 128
        count = -(-(shift + length) // 128)
        row = jnp.concatenate([vec_ref[first + n : first + n + 1] for n in range(count)], axis=1)
        if shift:
            row = pltpu.roll(jnp.broadcast_to(row, (8, count * 128)), count * 128 - shift, 1)[:1]
        return row

    def wide_row(at):
        lane = lax.broadcasted_iota(jnp.int32, (1, WIDE), 1)
        return jnp.where(lane < C3, vector_row(at, C3)[:, :WIDE], 0.0)

    gain2, bias2, scale2 = (vec_ref[n : n + 1] for n in range(3, 6))
    hid_bias = vector_row(6 * C2, HID2)
    out_bias = vector_row(6 * C2 + HID2, C2)
    two = 7 * C2 + HID2
    embed_bias, gain3, bias3, scale3 = (wide_row(two + n * C3) for n in range(4))
    gain4, bias4, scale4 = (wide_row(two + n * C3) for n in range(4, 7))
    hid_bias3 = vector_row(two + 7 * C3, HID3)[:, :HID3]
    out_bias3 = wide_row(two + 7 * C3 + HID3)
    mean2, scaling2 = stat_ref[2], stat_ref[3]
    factor2 = scaling2 * gain2
    shift2 = bias2 - mean2 * scaling2 * gain2
    for plane in range(4):
        zed_ref[plane, 0:LINE] = jnp.zeros((LINE, C2), f32)
    col3_ref[0:LINE] = jnp.zeros((LINE, WIDE), f32)
    col3_ref[AREA + LINE : AREA + 2 * LINE] = jnp.zeros((LINE, WIDE), f32)

    def put_block(number, block):
        near_ref[near_place[number]] = block
        far_ref[far_place[number]] = block

    def pack_blocks(matrices):
        offsets = [0]
        for rows, cols in SHAPES:
            offsets.append(offsets[-1] + rows // BS * (cols // BS))
        for which in matrices:
            (rows, cols), ref = SHAPES[which], grads[which]
            wide = cols // BS
            for rb in range(rows // BS):
                for cb in range(0, wide, 2):
                    number = offsets[which] + rb * wide + cb
                    at = slice(cb * BS, cb * BS + 128)
                    top = ref[rb * BS : rb * BS + HALF, at].astype(bf16)
                    low = ref[rb * BS + HALF : rb * BS + BS, at].astype(bf16)
                    put_block(number, jnp.where(left_half, top, pltpu.roll(low, BS, 1)))
                    if cb + 1 < wide:
                        put_block(number + 1, jnp.where(left_half, pltpu.roll(top, BS, 1), low))

    def plane_rows(plane):
        return slice(plane * AREA, plane * AREA + AREA)

    def begin_plane(plane):
        low = affine(mix_ref[plane], factor2, shift2).astype(bf16)
        h_ref[plane_rows(plane)] = low
        hid_ref[plane % 2] = product(low, w1_ref[...])

    begin_plane(0)
    for plane in range(4):
        if plane < 3:
            begin_plane(plane + 1)
        for k in range(STEPS):
            rows = step_rows(k)
            flat = slice(plane * AREA + k * STEP, plane * AREA + k * STEP + STEP)
            for at in range(0, HID2, 128):
                lanes = slice(at, at + 128)
                active, slope = gelu_pair(hid_ref[plane % 2, rows, lanes] + hid_bias[:, lanes])
                u_ref[flat, lanes] = active.astype(bf16)
                g_ref[flat, lanes] = slope.astype(bf16)
        out = product(u_ref[plane_rows(plane)], w2_ref[...]) + out_bias
        zed = jnp.where(inv_ref[plane] > 0.0, mix_ref[plane] + scale2 * out, 0.0)
        zed_ref[plane, LINE : LINE + AREA] = rounded(zed)

    def patches(k, carry):
        rows = step_rows(k)
        taps = []
        for ky in range(3):
            pr = (0 if ky == 1 else 1) * 2
            source = step_rows(k, 0 if ky == 0 else 1)
            even = zed_ref[pr, source]
            odd = zed_ref[pr + 1, source]
            taps.append((from_left(odd), even, odd))
        for ky in range(3):
            for kx in range(3):
                at = (3 * ky + kx) * C2
                tap = taps[ky][kx]
                if ky != kx:
                    tap = jnp.where(flipped, taps[kx][ky], tap)
                patch_ref[rows, at : at + C2] = tap.astype(bf16)
        return carry

    sweep(patches, 0)
    e_ref[...] = product(patch_ref[...], we_ref[...])

    def embed(k, carry):
        total, square = carry
        rows = step_rows(k)
        share = shape.share3(k)
        inv3_ref[rows] = share
        out = jnp.where(widen(share) > 0.0, e_ref[rows] + embed_bias, 0.0)
        e_ref[rows] = out
        return (total + fold(out), square + fold(out * out))

    total, square = sweep(embed, (nothing3, nothing3))
    mean3, scaling3 = norm_terms(total, square, count_three)
    factor3 = scaling3 * gain3
    shift3 = bias3 - mean3 * scaling3 * gain3

    def window_cols3(k, carry):
        rows = step_rows(k)
        normal = rounded(affine(e_ref[rows], factor3, shift3))
        masked = jnp.where(widen(inv3_ref[rows]) > 0.0, normal, 0.0)
        col3_ref[step_rows(k, 1)] = masked + from_left(masked) + from_right(masked)
        return carry

    sweep(window_cols3, 0)

    def row_windows3(k):
        return col3_ref[step_rows(k)] + col3_ref[step_rows(k, 1)] + col3_ref[step_rows(k, 2)]

    def mix3(k, carry):
        total, square = carry
        rows = step_rows(k)
        values = e_ref[rows]
        share = widen(inv3_ref[rows])
        pooled = row_windows3(k) * share - rounded(affine(values, factor3, shift3))
        pooled = jnp.where(share > 0.0, pooled, 0.0)
        mixed = values + scale3 * pooled
        pool3_ref[rows] = pooled
        mix3_ref[rows] = mixed
        return (total + fold(mixed), square + fold(mixed * mixed))

    total, square = sweep(mix3, (nothing3, nothing3))
    mean4, scaling4 = norm_terms(total, square, count_three)
    factor4 = scaling4 * gain4
    shift4 = bias4 - mean4 * scaling4 * gain4
    normal4 = (spread(scaling4, WIDE), spread(-mean4 * scaling4, WIDE))

    def prepare3(k, d_bias):
        rows = step_rows(k)
        h3_ref[rows] = affine(mix3_ref[rows], factor4, shift4).astype(bf16)
        goal = goal_ref[0, rows].astype(f32)
        goal = jnp.where(widen(inv3_ref[rows]) > 0.0, goal, 0.0)
        low_goal = (scale4 * goal).astype(bf16)
        dy3_ref[rows] = low_goal
        return d_bias + fold(low_goal.astype(f32))

    acc_three[7] += sweep(prepare3, nothing3)

    def keep(ref, value, place=slice(None)):
        if pairs == 1:
            ref[place] = value.astype(ref.dtype)
        else:

            @pl.when(pair == 0)
            def _():
                ref[place] = value

            @pl.when(pair > 0)
            def _():
                ref[place] += value

    def begin_chunk(at):
        lanes = slice(at, at + 256)
        hid3_ref[:, lanes] = product(h3_ref[...], w3_ref[:, lanes])
        dhid3_ref[:, lanes] = product_nt(dy3_ref[...], w4_ref[lanes])

    begin_chunk(0)
    for at in range(0, HID3, 256):
        if at + 256 < HID3:
            begin_chunk(at + 256)
        for lane in (at, at + 128):
            lanes = slice(lane, lane + 128)
            total = nothing
            for k in range(STEPS):
                rows = step_rows(k)
                active, slope = gelu_pair(hid3_ref[rows, lanes] + hid_bias3[:, lanes])
                u3_ref[rows, lanes] = active.astype(bf16)
                low = (slope * dhid3_ref[rows, lanes]).astype(bf16)
                g3_ref[rows, lanes] = low
                total = total + fold(low.astype(f32))
            acc_hid_three[:, lanes] += total
        lanes = slice(at, at + 256)
        out = product(u3_ref[:, lanes], w4_ref[lanes])
        d_low = product_nt(g3_ref[:, lanes], w3_ref[:, lanes])
        result_ref[0] = out if at == 0 else result_ref[0] + out
        dx3_ref[...] = d_low if at == 0 else dx3_ref[...] + d_low
        keep(gw3_ref, product_tn(h3_ref[...], g3_ref[:, lanes]), (slice(None), lanes))
        keep(gw4_ref, product_tn(u3_ref[:, lanes], dy3_ref[...]), lanes)

    def finish3(k, carry):
        d_scale, d_shift, d_gain = carry
        rows = step_rows(k)
        valid = widen(inv3_ref[rows]) > 0.0
        mixed = mix3_ref[rows]
        out = jnp.where(valid, result_ref[0, rows] + out_bias3, 0.0)
        result_ref[0, rows] = mixed + scale4 * out
        d_scale = d_scale + fold(out * goal_ref[0, rows].astype(f32))
        d_low = dx3_ref[rows]
        normal = affine(mixed, *normal4)
        return (d_scale, d_shift + fold(d_low), d_gain + fold(d_low * normal))

    d_scale, d_shift, d_gain = sweep(finish3, (nothing3, nothing3, nothing3))
    acc_three[6] += d_scale
    acc_three[5] += d_shift
    acc_three[4] += d_gain
    mean_shift = by_image(d_shift * gain4) / count_three
    mean_gain = by_image(d_gain * gain4) / count_three
    back_gain4 = scaling4 * gain4
    back_mean4 = spread(-scaling4 * mean_shift, WIDE)
    back_normal4 = spread(scaling4 * mean_gain, WIDE)

    def unmix3(k, d_scale):
        rows = step_rows(k)
        share = widen(inv3_ref[rows])
        valid = share > 0.0
        normal = affine(mix3_ref[rows], *normal4)
        back = affine(dx3_ref[rows], back_gain4, back_mean4) - scaled(normal, back_normal4)
        d_mixed = jnp.where(valid, back + goal_ref[0, rows].astype(f32), 0.0)
        dx3_ref[rows] = d_mixed
        d_scale = d_scale + fold(pool3_ref[rows] * d_mixed)
        weighted = scale3 * d_mixed * share
        col3_ref[step_rows(k, 1)] = weighted + from_left(weighted) + from_right(weighted)
        return d_scale

    acc_three[3] += sweep(unmix3, nothing3)
    normal3 = (spread(scaling3, WIDE), spread(-mean3 * scaling3, WIDE))

    def unpool3(k, carry):
        d_shift, d_gain = carry
        rows = step_rows(k)
        valid = widen(inv3_ref[rows]) > 0.0
        d_normal = jnp.where(valid, row_windows3(k) - scale3 * dx3_ref[rows], 0.0)
        pool3_ref[rows] = d_normal
        normal = affine(e_ref[rows], *normal3)
        return (d_shift + fold(d_normal), d_gain + fold(d_normal * normal))

    d_shift, d_gain = sweep(unpool3, (nothing3, nothing3))
    acc_three[2] += d_shift
    acc_three[1] += d_gain
    mean_shift = by_image(d_shift * gain3) / count_three
    mean_gain = by_image(d_gain * gain3) / count_three
    back_gain3 = scaling3 * gain3
    back_mean3 = spread(-scaling3 * mean_shift, WIDE)
    back_normal3 = spread(scaling3 * mean_gain, WIDE)

    def unnorm3(k, d_bias):
        rows = step_rows(k)
        valid = widen(inv3_ref[rows]) > 0.0
        normal = affine(e_ref[rows], *normal3)
        back = affine(pool3_ref[rows], back_gain3, back_mean3) - scaled(normal, back_normal3)
        low = jnp.where(valid, dx3_ref[rows] + back, 0.0).astype(bf16)
        dpre_ref[rows] = low
        return d_bias + fold(low.astype(f32))

    acc_three[0] += sweep(unnorm3, nothing3)
    keep(gwe_ref, product_tn(patch_ref[...], dpre_ref[...]))
    dpatch_ref[0:AREA] = product_nt(dpre_ref[...], we_ref[...])
    dpatch_ref[AREA : AREA + LINE] = jnp.zeros((LINE, 9 * C2), f32)

    def gather_back(k, carry):
        rows = step_rows(k)

        def tap(ky, kx, source):
            at = (3 * ky + kx) * C2
            value = dpatch_ref[source, at : at + C2]
            if ky != kx:
                at = (3 * kx + ky) * C2
                value = jnp.where(flipped, dpatch_ref[source, at : at + C2], value)
            return value

        sources = []
        for ky in range(3):
            source = step_rows(k, 1 if ky == 0 else 0)
            sources.append(
                (tap(ky, 1, source), tap(ky, 2, source) + from_right(tap(ky, 0, source)))
            )
        for pc in range(2):
            for pr, value in ((0, sources[1][pc]), (1, sources[2][pc] + sources[0][pc])):
                plane = pr * 2 + pc
                valid = inv_ref[plane, rows] > 0.0
                back_ref[plane, rows] = jnp.where(valid, rounded(value), 0.0)
        return carry

    sweep(gather_back, 0)

    if pairs == 1:
        pack_blocks(range(2, 5))

    normal2 = (spread(scaling2, C2), spread(-mean2 * scaling2, C2))

    def begin_back(plane):
        low_goal = (scale2 * back_ref[plane]).astype(bf16)
        dy_ref[plane_rows(plane)] = low_goal
        hid_ref[plane % 2] = product_nt(low_goal, w2_ref[...])
        return fold(low_goal.astype(f32))

    d_out_bias = begin_back(0)
    d_shift, d_gain = nothing, nothing
    sums = [nothing] * (HID2 // 128)
    new_gw1, new_gw2 = None, None
    for plane in range(4):
        if plane < 3:
            d_out_bias = d_out_bias + begin_back(plane + 1)
        for k in range(STEPS):
            rows = step_rows(k)
            part = slice(plane * AREA + k * STEP, plane * AREA + k * STEP + STEP)
            for n, at in enumerate(range(0, HID2, 128)):
                lanes = slice(at, at + 128)
                low = g_ref[part, lanes].astype(f32) * hid_ref[plane % 2, rows, lanes]
                low = low.astype(bf16)
                g_ref[part, lanes] = low
                sums[n] = sums[n] + fold(low.astype(f32))
        flat = plane_rows(plane)
        d_low = product_nt(g_ref[flat], w1_ref[...])
        dx_ref[plane] = d_low
        d_shift = d_shift + fold(d_low)
        d_gain = d_gain + fold(d_low * affine(mix_ref[plane], *normal2))
        part_gw1 = product_tn(h_ref[flat], g_ref[flat])
        part_gw2 = product_tn(dy_ref[flat], u_ref[flat])
        new_gw1 = part_gw1 if plane == 0 else new_gw1 + part_gw1
        new_gw2 = part_gw2 if plane == 0 else new_gw2 + part_gw2
    new_gw2 = new_gw2.T
    for n, value in enumerate(sums):
        acc_hid_two[:, n * 128 : n * 128 + 128] += value
    acc_two[6] += d_out_bias
    acc_two[4] += d_shift
    acc_two[3] += d_gain
    mean_out[0, 0] = spread(by_image(d_shift * gain2) / count_two, 128)
    mean_out[0, 1] = spread(by_image(d_gain * gain2) / count_two, 128)
    keep(gw1_ref, new_gw1)
    keep(gw2_ref, new_gw2)
    d_scale = fold(w2_ref[...].astype(f32) * new_gw2) + out_bias * d_out_bias
    acc_two[5] += d_scale / scale2

    def finish():
        if pairs > 1:
            pack_blocks(range(5))
        else:
            pack_blocks(range(2))

        def filler(number, carry):
            put_block(number, jnp.zeros((HALF, 128), bf16))
            return carry

        lax.fori_loop(USED, slots, filler, 0)

        flat_ref[...] = jnp.zeros(flat_ref.shape, f32)

        def put(at, total, length):
            if at % 128:
                room = jnp.zeros((8, 128), f32)
                if total.shape[1] < length + BS:
                    total = jnp.concatenate([total, room], axis=1)
                total = pltpu.roll(total, BS, 1)
            whole = jnp.sum(total, axis=0, keepdims=True)
            done = -(at % 128)
            row = at // 128
            lane = 0
            while done < length:
                first = max(0, -done)
                last = min(128, length - done)
                flat_ref[row : row + 1, first:last] = whole[:, lane + first : lane + last]
                done += 128
                lane += 128
                row += 1

        at = 3 * C2
        for n in range(3, 6):
            put(at, acc_two[n], C2)
            at += C2
        put(at, acc_hid_two[...], HID2)
        at += HID2
        put(at, acc_two[6], C2)
        at += C2
        for n in range(7):
            put(at, acc_three[n], C3)
            at += C3
        put(at, acc_hid_three[...], HID3)
        at += HID3
        put(at, acc_three[7], C3)

    at_pair(pairs - 1, finish)


def run_main(places, place, buckets, state, goal, vec, weights, strip_count):
    pairs = goal.shape[0]
    slots = places[0].shape[0]
    half = slots // 2 + 1
    if pairs == 1:
        state = held_in(pltpu.VMEM, *state)
    weights = held_in(pltpu.VMEM, *weights)
    _, inv, _, mix, stat = state
    state_shapes = [STATE[1], STATE[3], STATE[4]]
    grad_kind = bf16 if pairs == 1 else f32
    wide_f32 = pltpu.VMEM((AREA, WIDE), f32)
    wide_bf16 = pltpu.VMEM((AREA, WIDE), bf16)
    scratch = [
        pltpu.VMEM((4, AREA + LINE, C2), f32),
        pltpu.VMEM((2, AREA, HID2), f32),
        pltpu.VMEM((4 * AREA, HID2), bf16),
        pltpu.VMEM((4 * AREA, HID2), bf16),
        pltpu.VMEM((4 * AREA, C2), bf16),
        pltpu.VMEM((4 * AREA, C2), bf16),
        pltpu.VMEM((AREA, 9 * C2), bf16),
        pltpu.VMEM((AREA + LINE, 9 * C2), f32),
        pltpu.VMEM((AREA, 128), f32),
        wide_f32,
        pltpu.VMEM((AREA + 2 * LINE, WIDE), f32),
        wide_f32,
        wide_f32,
        wide_f32,
        pltpu.VMEM((AREA, HID3), f32),
        pltpu.VMEM((AREA, HID3), f32),
        pltpu.VMEM((AREA, HID3), bf16),
        pltpu.VMEM((AREA, HID3), bf16),
        wide_bf16,
        wide_bf16,
        wide_bf16,
        pltpu.VMEM((C2, HID2), grad_kind),
        pltpu.VMEM((HID2, C2), grad_kind),
        pltpu.VMEM((9 * C2, WIDE), grad_kind),
        pltpu.VMEM((WIDE, HID3), grad_kind),
        pltpu.VMEM((HID3, WIDE), grad_kind),
        pltpu.VMEM((7, 8, C2), f32),
        pltpu.VMEM((8, HID2), f32),
        pltpu.VMEM((8, 8, WIDE), f32),
        pltpu.VMEM((8, HID3), f32),
    ]
    out_shapes = [(half, HALF, 128), (half, HALF, 128), (VEC_BLOCKS * HALF, 128)]
    make = pltpu.VMEM if pairs == 1 else jax.ShapeDtypeStruct
    return pl.pallas_call(
        functools.partial(main_kernel, pairs, strip_count, slots),
        grid=() if pairs == 1 else (pairs,),
        in_specs=[SMEM] * 4
        + pair_specs(pairs, state_shapes + [goal.shape[1:]], pl.Buffered(1))
        + whole_specs(pairs, [vec.shape])
        + [VMEM_BLOCK] * 5,
        out_specs=pair_specs(pairs, [(AREA, WIDE)] + BACK) + whole_specs(pairs, out_shapes),
        out_shape=pair_arrays(pairs, [(AREA, WIDE)] + BACK, [f32] * 4)
        + [make(shape, kind) for shape, kind in zip(out_shapes, (bf16, bf16, f32))],
        scratch_shapes=scratch,
        compiler_params=pltpu.CompilerParams(
            vmem_limit_bytes=(40 if pairs == 1 else 56) * 1024 * 1024,
            fuse_transposed_lhs_in_matmul=True,
        ),
        name="blocks",
    )(*places, place, buckets, inv, mix, stat, goal, vec, *weights)


def exit_kernel(
    pairs,
    strip_count,
    place_ref,
    bucket_ref,
    x_in,
    inv_in,
    pool_in,
    mix_in,
    stat_in,
    zed_in,
    dx_in,
    mean_in,
    flat_ref,
    vec_ref,
    payload_hbm,
    vector_ref,
    payload_ref,
    image_ref,
    col_ref,
    dx_ref,
    back_ref,
    acc_ref,
    sem,
):
    pair = pl.program_id(0) if pairs > 1 else 0
    x_ref, inv_ref, pool_ref, mix_ref, stat_ref, zed_ref, low_ref, mean_ref = (
        ref.at[0] for ref in (x_in, inv_in, pool_in, mix_in, stat_in, zed_in, dx_in, mean_in)
    )
    bucket_of = bucket_reader(place_ref, bucket_ref, strip_count)
    shape = Geometry(bucket_of, pair)
    count_two = shape.count_two
    gain1, bias1, scale1, gain2 = (vec_ref[n : n + 1] for n in range(4))
    mean1, scaling1, mean2, scaling2 = (stat_ref[n] for n in range(4))
    normal2 = (scaling2, -mean2 * scaling2)
    clear_edges(col_ref)
    nothing = jnp.zeros((8, C2), f32)
    back_gain2 = scaling2 * gain2
    back_mean2 = -scaling2 * mean_ref[0]
    back_normal2 = scaling2 * mean_ref[1]

    if pairs > 1:

        @pl.when(pair == 0)
        def _():
            acc_ref[...] = jnp.zeros(acc_ref.shape, f32)

    def add_up(n, total):
        acc_ref[n] = total if pairs == 1 else acc_ref[n] + total

    def unmix(k, d_scale):
        rows = step_rows(k)
        for pr in range(2):
            weighted = []
            for pc in range(2):
                plane = pr * 2 + pc
                share = inv_ref[plane, rows]
                normal = affine(mix_ref[plane, rows], *normal2)
                back = affine(low_ref[plane, rows], back_gain2, back_mean2)
                back = back - scaled(normal, back_normal2)
                d_mixed = jnp.where(share > 0.0, zed_ref[plane, rows] + back, 0.0)
                dx_ref[plane, rows] = d_mixed
                d_scale = d_scale + fold(pool_ref[plane, rows] * d_mixed)
                weighted.append(scale1 * d_mixed * share)
            put_col_windows(col_ref, pr, k, *weighted)
        return d_scale

    add_up(2, sweep(unmix, nothing))
    normal1 = (spread(scaling1, C2), spread(-mean1 * scaling1, C2))

    def unpool(k, carry):
        d_shift, d_gain = carry
        rows = step_rows(k)
        for pc in range(2):
            windows = row_windows(col_ref, pc, k)
            for pr in range(2):
                plane = pr * 2 + pc
                valid = inv_ref[plane, rows] > 0.0
                d_normal = windows[pr] - scale1 * dx_ref[plane, rows]
                d_normal = jnp.where(valid, d_normal, 0.0)
                back_ref[plane, rows] = d_normal
                normal = affine(x_ref[plane, rows], *normal1)
                d_shift = d_shift + fold(d_normal)
                d_gain = d_gain + fold(d_normal * normal)
        return (d_shift, d_gain)

    d_shift, d_gain = sweep(unpool, (nothing, nothing))
    add_up(1, d_shift)
    add_up(0, d_gain)
    mean_shift = by_image(d_shift * gain1) / count_two
    mean_gain = by_image(d_gain * gain1) / count_two
    back_gain1 = scaling1 * gain1
    back_mean1 = spread(-scaling1 * mean_shift, C2)
    back_normal1 = spread(scaling1 * mean_gain, C2)

    def unnorm(k, carry):
        rows = step_rows(k)
        for plane in range(4):
            normal = affine(x_ref[plane, rows], *normal1)
            back = affine(back_ref[plane, rows], back_gain1, back_mean1)
            back = back - scaled(normal, back_normal1)
            valid = inv_ref[plane, rows] > 0.0
            dx_ref[plane, rows] = jnp.where(valid, dx_ref[plane, rows] + back, 0.0)
        return carry

    sweep(unnorm, 0)

    def give_back(plane, here, spot, there):
        image_ref[spot, there] = dx_ref[plane, here]

    image_ref[...] = jnp.zeros(image_ref.shape, f32)
    each_image(bucket_of, pair, give_back)

    for spot in range(2 * STRIPS):
        target = strip_place(pair, spot, strip_count)
        for within in range(SR):
            rows = slice(within * CW, within * CW + CW)
            payload_ref[target, within] = image_ref[spot, rows].astype(bf16)

    def finish():
        copy = pltpu.make_async_copy(payload_ref, payload_hbm, sem)
        copy.start()
        vector_ref[...] = flat_ref[...]
        for n in range(3):
            vector_ref[n : n + 1] = jnp.sum(acc_ref[n], axis=0, keepdims=True)
        copy.wait()

    if pairs == 1:
        finish()
    else:
        pl.when(pair == pairs - 1)(finish)


def run_exit(place, buckets, state, back, flat, vec, strip_count):
    pairs = strip_count // 8
    payload = (strip_count, SR, CW, C2)
    make = pltpu.VMEM if pairs == 1 else jax.ShapeDtypeStruct
    plane_f32 = pltpu.VMEM((4, AREA, C2), f32)
    arrays = [*state, *back]
    if pairs == 1:
        arrays = held_in(pltpu.VMEM, *arrays)
    return pl.pallas_call(
        functools.partial(exit_kernel, pairs, strip_count),
        grid=() if pairs == 1 else (pairs,),
        in_specs=[SMEM] * 2
        + pair_specs(pairs, STATE + BACK, pl.Buffered(1))
        + whole_specs(pairs, [flat.shape, vec.shape]),
        out_specs=[HBM] + whole_specs(pairs, [flat.shape]),
        out_shape=[pltpu.HBM(payload, bf16), make(flat.shape, f32)],
        scratch_shapes=[
            pltpu.VMEM(payload, bf16),
            pltpu.VMEM((2 * STRIPS, STRIP_ROWS, C2), f32),
            pltpu.VMEM((4, AREA + 2 * LINE, C2), f32),
            plane_f32,
            plane_f32,
            pltpu.VMEM((3, 8, C2), f32),
            pltpu.SemaphoreType.DMA,
        ],
        compiler_params=roomy(8 if pairs == 1 else 40),
        name="exit",
    )(place, buckets, *arrays, flat, vec)


def dense_blocks(values):
    return jnp.concatenate([values[:, :HALF], values[:, HALF:]], axis=2).astype(bf16)


def pack_kernel(master_ref, dense_ref):
    dense_ref[...] = dense_blocks(master_ref[...])


def pack(master):
    owned = master.shape[0]
    return pl.pallas_call(
        pack_kernel,
        out_shape=jax.ShapeDtypeStruct((owned, HALF, 2 * BS), bf16),
        name="pack",
    )(master)


def halves_of(owned):
    return [(0, (owned + 1) // 2), ((owned + 1) // 2, owned // 2)]


def pack_pieces_kernel(place_ref, master_hbm, pixel_hbm, *refs):
    out_refs, (wide_ref, master_ref, pixel_ref, sem) = refs[:6], refs[6:]
    owned = master_ref.shape[0]
    slots = pixel_ref.shape[2]
    copies = [pltpu.make_async_copy(pixel_hbm, pixel_ref, sem.at[0])]
    parts = halves_of(owned)
    for n, part in enumerate(parts):
        copies.append(
            pltpu.make_async_copy(
                master_hbm.at[pl.ds(*part)], master_ref.at[pl.ds(*part)], sem.at[1 + n]
            )
        )
    for copy in copies:
        copy.start()
    copies[0].wait()

    def widen_row(row, carry):
        start = pl.multiple_of(row * CW * slots, 8)
        values = pixel_ref[row].astype(f32).reshape(CW * slots, C2)
        wide_ref[pl.ds(start, CW * slots)] = values
        return carry

    lax.fori_loop(0, SR, widen_row, 0)
    own_ref, x_ref, x_late_ref, y_ref, y_late_ref, both_ref = out_refs
    for k, ref in enumerate((own_ref, x_ref, y_ref, both_ref)):
        for other in range(2):
            slot = place_ref[0] ^ (2 * k + other)
            first = other * (ref.shape[0] - STRIP_ROWS)
            strip = wide_ref[pl.ds(slot, STRIP_ROWS, stride=slots)]
            ref[first : first + STRIP_ROWS] = strip.astype(bf16)
    targets = ((x_ref, y_late_ref), (y_ref, x_late_ref))
    for (first, count), copy, (early_ref, late_ref) in zip(parts, copies[1:], targets):
        copy.wait()
        rows = count * HALF
        dense = dense_blocks(master_ref[first : first + count]).reshape(rows, 2 * BS)
        own_ref[STRIP_ROWS + first * HALF : STRIP_ROWS + first * HALF + rows] = dense
        early_ref[STRIP_ROWS : STRIP_ROWS + rows] = dense
        late_ref[...] = dense


def pack_pieces(place, master, pixels):
    slots = pixels.shape[2]
    first, second = (count * HALF for _, count in halves_of(master.shape[0]))
    strips = 2 * STRIP_ROWS
    rows = (strips + first + second, strips + first, second, strips + second, first, strips)
    shapes = [(count, 2 * BS) for count in rows]
    return pl.pallas_call(
        pack_pieces_kernel,
        in_specs=[SMEM] + [HBM] * 2,
        out_specs=[VMEM_BLOCK] * 6,
        out_shape=[pltpu.VMEM(shape, bf16) for shape in shapes],
        scratch_shapes=[
            pltpu.VMEM((STRIP_ROWS * slots, C2), f32),
            pltpu.VMEM(master.shape, f32),
            pltpu.VMEM(pixels.shape, bf16),
            pltpu.SemaphoreType.DMA((3,)),
        ],
        compiler_params=roomy(12),
        name="pack",
    )(place, *held_in(pltpu.HBM, master, pixels))


def fold_pair_kernel(near_ref, got_ref, own_ref, *part_refs):
    share = own_ref.shape[0]

    def one(n, carry):
        own_ref[n] = near_ref[n].astype(f32) + got_ref[n].astype(f32)
        for k, ref in enumerate(part_refs):
            here = (k + 1) * share + n
            ref[n] = near_ref[here] + got_ref[here]
        return carry

    lax.fori_loop(0, share, one, 0, unroll=4)


def fold_pair(near, got, groups):
    shape = ((near.shape[0] - 1) // groups,) + near.shape[1:]
    return pl.pallas_call(
        fold_pair_kernel,
        in_specs=[VMEM_BLOCK] * 2,
        out_specs=[VMEM_BLOCK] * groups,
        out_shape=[pltpu.VMEM(shape, f32)] + [pltpu.VMEM(shape, bf16)] * (groups - 1),
        compiler_params=roomy(4),
        name="fold_pair",
    )(*held_in(pltpu.VMEM, near, got))


def fold_tile_kernel(pieces, spot_ref, *refs):
    piece_refs, refs = refs[:pieces], refs[pieces:]
    vector_refs, refs = refs[:pieces], refs[pieces:]
    out_refs, sum_ref = refs[:-1], refs[-1]
    groups = len(out_refs)
    share = out_refs[0].shape[0]
    owned = piece_refs[0].shape[0]
    total = vector_refs[0][...]
    for ref in vector_refs[1:]:
        total = total + ref[...]
    for n in range(sum_ref.shape[0]):
        sum_ref[n] = jnp.zeros((HALF, 128), f32)
    for n in range(VEC_BLOCKS):
        sum_ref[n] = total[n * HALF : (n + 1) * HALF]

    def one(n, carry):
        for k, out_ref in enumerate(out_refs):
            number = lax.rem(spot_ref[0] + k, groups) * share + n
            block = jnp.minimum(number, owned - 1)
            total = piece_refs[0][block].astype(f32)
            for ref in piece_refs[1:]:
                total = total + ref[block].astype(f32)
            rest = sum_ref[jnp.maximum(number - owned, 0)]
            out_ref[n] = jnp.where(number < owned, total, rest).astype(out_ref.dtype)
        return carry

    lax.fori_loop(0, share, one, 0, unroll=share <= 16)


def fold_tile(spot, pieces, vectors, extra, groups):
    shape = ((pieces[0].shape[0] + extra) // groups,) + pieces[0].shape[1:]
    return pl.pallas_call(
        functools.partial(fold_tile_kernel, len(pieces)),
        in_specs=[SMEM] + [VMEM_BLOCK] * (len(pieces) + len(vectors)),
        out_specs=[VMEM_BLOCK] * groups,
        out_shape=[pltpu.VMEM(shape, f32)] + [pltpu.VMEM(shape, bf16)] * (groups - 1),
        scratch_shapes=[pltpu.VMEM((extra, HALF, 128), f32)],
        compiler_params=roomy(8),
        name="fold_tile",
    )(spot, *held_in(pltpu.VMEM, *pieces, *vectors))


def fold_batch_kernel(owned, vector_weight, spot_ref, *refs):
    part_refs, (total_ref, norm_ref) = refs[:-2], refs[-2:]
    share = total_ref.shape[0]
    square = jnp.zeros((8, 128), f32)
    for n in range(share):
        total = part_refs[0][n].astype(f32)
        for ref in part_refs[1:]:
            total = total + ref[n].astype(f32)
        total_ref[n] = total.astype(bf16)
        weight = jnp.where(spot_ref[0] * share + n < owned, 1.0, vector_weight)
        square = square + weight * fold(total * total)
    square = jnp.sum(jnp.sum(square, axis=1, keepdims=True), axis=0, keepdims=True)
    norm_ref[...] = jnp.broadcast_to(square[None], norm_ref.shape)


def fold_batch(spot, parts, owned, tile_count):
    count = tile_count * len(parts)
    return pl.pallas_call(
        functools.partial(fold_batch_kernel, owned, 1.0 / tile_count),
        in_specs=[SMEM] + [VMEM_BLOCK] * len(parts),
        out_specs=[VMEM_BLOCK] * 2,
        out_shape=[pltpu.VMEM(parts[0].shape, bf16), pltpu.VMEM((count, 1, 128), f32)],
        name="fold_batch",
    )(spot, *held_in(pltpu.VMEM, *parts))


def update_kernel(owned, groups, spot_ref, norm_ref, *refs):
    quarters, refs = refs[:groups], refs[groups:]
    stat_hbm, out_hbm, (vector_ref, clip_ref), refs = refs[:5], refs[5:10], refs[10:12], refs[12:]
    stat_refs, out_refs, (in_sem, out_sem) = refs[:5], refs[5:10], refs[10:]
    master_ref, left_stat_ref, right_stat_ref, left_root_ref, right_root_ref = stat_refs
    grad_ref, left_ref, right_ref, new_ref, copy_ref = out_refs
    share = quarters[0].shape[0]
    spans = spans_of(owned)

    def copies_of(sources, targets, sems):
        return [
            [
                pltpu.make_async_copy(
                    source.at[pl.ds(*span)], target.at[pl.ds(*span)], sems.at[5 * n + k]
                )
                for k, (source, target) in enumerate(zip(sources, targets))
            ]
            for n, span in enumerate(spans)
        ]

    copies_in = copies_of(stat_hbm, stat_refs, in_sem)
    copies_out = copies_of(out_refs, out_hbm, out_sem)
    for copies in copies_in:
        for copy in copies:
            copy.start()
    norm = jnp.sqrt(jnp.sum(norm_ref[...], axis=0))
    factor = jnp.minimum(1.0, clip_limit / norm)
    left_half = lax.broadcasted_iota(jnp.int32, (HALF, 128), 1) < BS

    def summed(number):
        source = number // share
        local = number - source * share
        turn = lax.rem(spot_ref[0] - source + groups, groups)
        value = quarters[0][local].astype(f32)
        for k in range(1, groups):
            value = jnp.where(turn == k, quarters[k][local].astype(f32), value)
        return value * factor

    def side_by_side(first, count):
        sides = []
        for n in range(first, first + count, 2):
            dense = summed(n)
            turned = pltpu.roll(dense, BS, 1)
            if n + 1 < first + count:
                second = summed(n + 1)
                top = jnp.where(left_half, dense, pltpu.roll(second, BS, 1))
                low = jnp.where(left_half, turned, second)
                side = jnp.concatenate([top, low], axis=0)
                grad_ref[n + 1] = pltpu.roll(side, BS, 1)[:, :BS]
            else:
                side = jnp.concatenate([dense, turned], axis=0)[:, :BS]
            grad_ref[n] = side[:, :BS]
            sides.append(side.astype(bf16))
        return jnp.concatenate(sides, axis=1)

    def diagonal_of(count):
        order = (count * BS, count * BS)
        return lax.broadcasted_iota(jnp.int32, order, 0) // BS == (
            lax.broadcasted_iota(jnp.int32, order, 1) // BS
        )

    clip_ref[...] = norm
    for n in range(vector_ref.shape[0]):
        vector_ref[n] = summed(owned + n)
    for (first, length), arriving, leaving in zip(spans, copies_in, copies_out):
        parts = [(n, min(4, first + length - n)) for n in range(first, first + length, 4)]
        wides = [side_by_side(*part) for part in parts]
        tall = [
            jnp.where(diagonal_of(count), jnp.concatenate([wide] * count, axis=0), 0.0)
            for (_, count), wide in zip(parts, wides)
        ]
        lefts = [product_nt(one, wide) for one, wide in zip(tall, wides)]
        rights = [product_tn(wide, wide) for wide in wides]
        for copy in arriving:
            copy.wait()
        stepped = []
        for (start, count), wide in zip(parts, wides):
            roots = left_root_ref[pl.ds(start, count)].reshape(count * BS, BS).astype(bf16)
            stepped.append(product(roots, wide))
        for (start, count), left, right in zip(parts, lefts, rights):
            here = pl.ds(start, count)
            left_ref[here] = 0.5 * left_stat_ref[here] + 0.5 * left.reshape(count, BS, BS)
            for n in range(count):
                at = n // 2 * 128
                block = right[n * BS : n * BS + BS, at : min(at + 128, count * BS)]
                if n % 2:
                    block = pltpu.roll(block, BS, 1)
                right_ref[start + n] = 0.5 * right_stat_ref[start + n] + 0.5 * block[:, :BS]
        for (start, count), value in zip(parts, stepped):
            here = pl.ds(start, count)
            value = jnp.where(diagonal_of(count), value, 0.0).astype(bf16)
            roots = right_root_ref[here].reshape(count * BS, BS).astype(bf16)
            value = product(value, roots).reshape(count, BS, BS)
            new = master_ref[here] - rate_matrix * value
            new_ref[here] = new
            copy_ref[here] = new.astype(bf16)
        for copy in leaving:
            copy.start()
    for leaving in copies_out:
        for copy in leaving:
            copy.wait()


def spans_of(owned):
    spans = []
    first = 0
    while first < owned:
        length = min(8 if first == 0 else 12, owned - first)
        spans.append((first, length))
        first += length
    return spans


def update(spot, norm, quarters, extra, *stats):
    shape = stats[0].shape
    groups = len(quarters)
    types = [f32] * 4 + [bf16]
    steps = len(spans_of(shape[0]))
    return pl.pallas_call(
        functools.partial(update_kernel, shape[0], groups),
        in_specs=[SMEM] + [VMEM_BLOCK] * (groups + 1) + [HBM] * 5,
        out_specs=[HBM] * 5 + [VMEM_BLOCK] * 2,
        out_shape=[pltpu.HBM(shape, kind) for kind in types]
        + [
            pltpu.VMEM((extra, HALF, 128), f32),
            pltpu.VMEM((1, 128), f32),
        ],
        scratch_shapes=[pltpu.VMEM(shape, f32)] * 5
        + [pltpu.VMEM(shape, kind) for kind in types]
        + [
            pltpu.SemaphoreType.DMA((5 * steps,)),
            pltpu.SemaphoreType.DMA((5 * steps,)),
        ],
        compiler_params=roomy(20),
        name="update",
    )(spot, *held_in(pltpu.VMEM, norm, *quarters), *held_in(pltpu.HBM, *stats))


def share_out(pieces, axis):
    return lax.all_to_all(pieces, axis, split_axis=0, concat_axis=0, tiled=True)


def swap(piece, distance):
    count = lax.axis_size("tile")
    return lax.ppermute(piece, "tile", [(i, i ^ distance) for i in range(count)])


def on_device(
    pixels,
    buckets,
    slot_owner_table,
    out_grad,
    master,
    left_stat,
    right_stat,
    left_root,
    right_root,
    vectors,
    moment,
):
    tile_count = lax.axis_size("tile")
    tile_place = lax.axis_index("tile")
    slot_count = pixels.shape[2]
    group_count = tile_count // STRIPS
    pairs = group_count // 2
    owned = master.shape[0]
    slots = owned * tile_count
    batch_count = lax.axis_size("batch")
    spot = lax.axis_index("batch").astype(jnp.int32).reshape(1)
    extra = extra_of(owned, batch_count)
    place = tile_place.astype(jnp.int32).reshape(1)
    paired = tile_count == 8
    numbers = jnp.arange(slots, dtype=jnp.int32)
    slot_of = jnp.sum(
        jnp.where(slot_owner_table[None, :] == numbers[:, None], numbers[None, :], 0), axis=1
    )
    if paired:
        owner = slot_of // owned
        apart = owner ^ tile_place
        apart = (apart & 1) * (tile_count // 2) + (apart >> 1)
        slot_of = slot_of + owned * (apart - owner)
    half = slots // 2
    near_place = jnp.where(slot_of < half, slot_of, half)
    far_place = jnp.where(slot_of < half, half, slot_of - half)
    vec = vectors.reshape(-1, 128)
    turned = lax.dynamic_index_in_dim(
        buckets.reshape(group_count, slot_count), tile_place, 1, keepdims=False
    ) >= 2
    flips = turned.reshape(-1, 1, 1, 1)
    goal = out_grad.reshape(2 * pairs, H3, W3, C3)
    goal = jnp.where(flips, goal.transpose(0, 2, 1, 3), goal)[:, :LINES]
    goal = goal.reshape(pairs, 2, LINES, W3, C3).transpose(0, 2, 3, 1, 4)
    goal = goal.reshape(pairs, LINES, 2 * W3, C3)
    goal = jnp.pad(goal, ((0, 0), (0, 0), (0, LINE - 2 * W3), (0, WIDE - C3)))
    goal = goal.reshape(pairs, AREA, WIDE)

    if paired:
        own, for_x, for_x_late, for_y, for_y_late, for_both = pack_pieces(
            place, master, pixels[0, 0].transpose(1, 2, 0, 3)
        )
        goal, vec, slot_of, near_place, far_place, own = lax.optimization_barrier(
            (goal, vec, slot_of, near_place, far_place, own)
        )
        from_x, from_y = swap(for_x, 2), swap(for_y, 4)
        first_half = swap(from_x[STRIP_ROWS:-STRIP_ROWS], 4)
        second_half = swap(from_y[STRIP_ROWS:-STRIP_ROWS], 2)
        strips_both = swap(for_both, 6)
        x_late, y_late = swap(for_x_late, 2), swap(for_y_late, 4)
        mine = [own, from_x, from_y, strips_both]
        theirs = [swap(piece, 1) for piece in mine]
        strips = mine + theirs
        late = [x_late, y_late, first_half, second_half]
        pieces, spans = [], []
        (_, first), (_, second) = halves_of(owned)
        for early, rest in ((mine, late), (theirs, [swap(piece, 1) for piece in late])):
            pieces += [early[0], early[1], rest[0], rest[1], early[2], rest[2], rest[3]]
            spans += [(STRIP_ROWS, owned), (STRIP_ROWS, first), (0, second)]
            spans += [(0, first), (STRIP_ROWS, second), (0, first), (0, second)]
    else:
        pieces = [lax.all_gather(pack(master), "tile", axis=0, tiled=True).reshape(-1, 2 * BS)]
        spans = [(0, slots)]
        strips = share_out(pixels.reshape(tile_count, STRIP, C2), "tile")
        strips = [jnp.pad(strips, ((0, 0), (0, STRIP_ROWS - STRIP), (0, 0)))]

    weights = run_unpack(slot_of, pieces, spans)
    state = run_entry(place, buckets, strips, vec, tile_count)
    result, *back, near, far, flat = run_main(
        (near_place, far_place),
        place,
        buckets,
        state,
        goal,
        vec,
        weights,
        tile_count,
    )
    pixel_back, vector = run_exit(place, buckets, state, back, flat, vec, tile_count)
    if paired:
        own, *parts = fold_pair(near, swap(far, 1), tile_count // 2)
        pieces = [own] + [swap(part, 2 * k + 2) for k, part in enumerate(parts)]
        vector, _ = lax.optimization_barrier((vector, parts[0]))
        vector = vector + swap(vector, 1)
        vectors_in = [vector] + [swap(vector, 2 * k) for k in range(1, tile_count // 2)]
    else:
        outgoing = jnp.concatenate([near[:half], far[:half]], axis=0)
        pieces = list(share_out(outgoing.reshape(tile_count, owned, HALF, 128), "tile"))
        vectors_in = list(lax.all_gather(vector, "tile"))
    result, pieces[1] = lax.optimization_barrier((result, pieces[1]))
    result = result.reshape(pairs, LINES, LINE, WIDE)[:, :, : 2 * W3, :C3]
    result = result.reshape(pairs, LINES, W3, 2, C3).transpose(0, 3, 1, 2, 4)
    result = result.reshape(2 * pairs, LINES, W3, C3)
    result = jnp.pad(result, ((0, 0), (0, H3 - LINES), (0, 0), (0, 0)))
    result = jnp.where(flips, result.transpose(0, 2, 1, 3), result)
    result = result.reshape(out_grad.shape)
    result = with_layout_constraint(result, Layout(major_to_minor=(0, 1, 2, 4, 5, 3, 6)))
    result, vectors_in[0] = lax.optimization_barrier((result, vectors_in[0]))
    own, *parts = fold_tile(spot, pieces, vectors_in, extra, batch_count)
    pixel_back, parts[0] = lax.optimization_barrier((pixel_back, parts[0]))
    returned = share_out(pixel_back, "tile")
    parts = [
        lax.ppermute(part, "batch", [(i, (i + k + 1) % batch_count) for i in range(batch_count)])
        for k, part in enumerate(parts)
    ]
    quarter, norm = fold_batch(spot, [own] + parts, owned, tile_count)
    returned, norm = lax.optimization_barrier((returned, norm))
    norm = share_out(norm, ("batch", "tile"))
    returned = returned.astype(f32).reshape(pixels.shape)
    returned = with_layout_constraint(returned, Layout(major_to_minor=(0, 1, 3, 4, 2, 5)))
    returned, quarter = lax.optimization_barrier((returned, quarter))
    quarters = [quarter] + [
        lax.ppermute(quarter, "batch", [(i, (i + k) % batch_count) for i in range(batch_count)])
        for k in range(1, batch_count)
    ]
    block_grad, left_new, right_new, master_new, weight_copy, whole_vector, clip = update(
        spot, norm, quarters, extra, master, left_stat, right_stat, left_root, right_root
    )
    clip_norm = clip[0, 0]
    share = vectors.shape[0] // tile_count
    whole_vector = whole_vector.reshape(-1)
    vec_grad = lax.dynamic_slice_in_dim(whole_vector, tile_place * share, share, 0)
    vec_moment = moment + vec_grad * vec_grad
    own_vectors = lax.dynamic_slice_in_dim(vectors, tile_place * share, share, 0)
    vec_new = own_vectors - rate_vector * vec_grad / (jnp.sqrt(vec_moment) + eps_adagrad)
    return (
        result,
        returned,
        clip_norm,
        block_grad,
        left_new,
        right_new,
        master_new,
        weight_copy,
        vec_grad,
        vec_moment,
        vec_new,
    )


def solution(mesh):
    placed = (
        P("batch", "tile", None, None, None, None),
        P("batch"),
        P(),
        P("batch", "tile", None, None, None, None, None),
        P("tile", None, None),
        P("tile", None, None),
        P("tile", None, None),
        P("tile", None, None),
        P("tile", None, None),
        P(),
        P("tile"),
    )
    return jax.shard_map(
        on_device,
        mesh=mesh,
        in_specs=placed,
        out_specs=(
            P("batch", "tile", None, None, None, None, None),
            P("batch", "tile", None, None, None, None),
            P(),
            P("tile", None, None),
            P("tile", None, None),
            P("tile", None, None),
            P("tile", None, None),
            P("tile", None, None),
            P("tile"),
            P("tile"),
            P("tile"),
        ),
        check_vma=False,
    )
```

```python
import functools

import jax
import jax.numpy as jnp
from jax import lax
from jax.experimental import pallas as pl
from jax.experimental.layout import Layout, with_layout_constraint
from jax.experimental.pallas import tpu as pltpu
from jax.sharding import PartitionSpec as P

C2 = 128
HID2 = 512
C3 = 320
HID3 = 1280
CH = 36
CW = 36
STRIPS = 4
BS = 64
SR = CH // STRIPS
H3 = CH // 2
W3 = CW // 2
LONG = 7 * CH // 9
LINES = LONG // 2
WIDE = 384
LINE = 40
AREA = LINES * LINE
STEP = 2 * LINE
STEPS = AREA // STEP
HALF = BS // 2
STRIP = SR * CW
STRIP_ROWS = STRIP + -STRIP % 16

eps_norm = 1e-05
clip_limit = 1.0
rate_matrix = 0.3
rate_vector = 0.3
eps_adagrad = 1e-08
f32 = jnp.float32
bf16 = jnp.bfloat16

SHAPES = [(C2, HID2), (HID2, C2), (9 * C2, C3), (C3, HID3), (HID3, C3)]
USED = sum(rows // BS * (cols // BS) for rows, cols in SHAPES)
VEC_ROWS = (6 * C2 + HID2 + C2 + C3 + 6 * C3 + HID3 + C3) // 128


VEC_BLOCKS = -(-VEC_ROWS // HALF)


def extra_of(owned, groups):
    return VEC_BLOCKS + -(owned + VEC_BLOCKS) % groups


def product(left, right):
    return jnp.dot(left, right, preferred_element_type=f32)


def product_nt(left, right):
    return lax.dot_general(left, right, (((1,), (1,)), ((), ())), preferred_element_type=f32)


def product_tn(left, right):
    return lax.dot_general(left, right, (((0,), (0,)), ((), ())), preferred_element_type=f32)


def gelu_pair(values):
    bell = jnp.exp2(values * values * (-0.5 * 1.4426950408889634))
    step = pl.reciprocal(1.0 + (0.3275911 * 0.7071067811865476) * jnp.abs(values), approx=True)
    tail = step * (
        0.5 * 0.254829592
        + step
        * (
            0.5 * -0.284496736
            + step
            * (0.5 * 1.421413741 + step * (0.5 * -1.453152027 + step * (0.5 * 1.061405429)))
        )
    )
    tail = tail * bell
    share = jnp.where(values >= 0.0, 1.0 - tail, tail)
    return (values * share, share + values * (bell * 0.3989422804014327))


def fold(values):
    chans = values.shape[-1]
    return jnp.sum(values.reshape(-1, 8, chans), axis=0)


def by_image(total):
    total = total + pltpu.roll(total, 4, 0)
    total = total + pltpu.roll(total, 2, 0)
    return jnp.sum(total, axis=1, keepdims=True)


def line(pattern):
    return jnp.concatenate([pattern] * (LINE // 8), axis=0)


def spread(pattern, chans):
    return jnp.broadcast_to(pattern, (8, chans))


def affine(values, factor, shift):
    tiles = values.reshape(-1, 8, values.shape[-1])
    return (tiles * factor + shift).reshape(values.shape)


def scaled(values, factor):
    tiles = values.reshape(-1, 8, values.shape[-1])
    return (tiles * factor).reshape(values.shape)


def from_left(values):
    return pltpu.roll(values, 2, 0)


def from_right(values):
    return pltpu.roll(values, values.shape[0] - 2, 0)


def rounded(values):
    return values.astype(bf16).astype(f32)


def widen(values):
    return jnp.concatenate([values] * (WIDE // 128), axis=-1)


def norm_terms(total, square, count):
    mean = by_image(total) / count
    scaling = lax.rsqrt(by_image(square) / count - mean * mean + eps_norm)
    return (mean, scaling)


def sweep(visit, start):
    return lax.fori_loop(0, STEPS, visit, start, unroll=True)


def step_rows(k, lines=0):
    start = k * STEP + lines * LINE
    return pl.ds(start if isinstance(k, int) else pl.multiple_of(start, LINE), STEP)


def held_in(space, *arrays):
    return [pltpu.with_memory_space_constraint(array, space) for array in arrays]


VMEM_BLOCK = pl.BlockSpec(memory_space=pltpu.VMEM)
HBM = pl.BlockSpec(memory_space=pltpu.HBM)
SMEM = pl.BlockSpec(memory_space=pltpu.SMEM)


def roomy(mebibytes):
    return pltpu.CompilerParams(vmem_limit_bytes=mebibytes * 1024 * 1024)


def image_shape(bucket_of, pair, image):
    bucket = bucket_of(2 * pair + image)
    plain = jnp.where(bucket == 0, 5 * CH // 9, 7 * CH // 9)
    across = jnp.where(bucket == 0, CW, 7 * CW // 9)
    turned = (bucket >= 2).astype(jnp.int32)
    return (
        jnp.where(turned > 0, 5 * CW // 9, plain),
        jnp.where(turned > 0, CH, across),
        turned,
    )


def bucket_reader(place_ref, bucket_ref, strip_count):
    return lambda group: bucket_ref[group * strip_count + place_ref[0]]


class Geometry:
    def __init__(self, bucket_of, pair):
        parity = lax.broadcasted_iota(jnp.int32, (8, 128), 0) % 2
        even, odd = (image_shape(bucket_of, pair, image) for image in range(2))
        high, broad, turned = (jnp.where(parity == 0, a, b) for a, b in zip(even, odd))
        self.high = high
        self.count_two = (high * broad * C2).astype(f32)[:, :1]
        self.high3 = (high + 1) // 2
        broad3 = (broad + 1) // 2
        self.count_three = (self.high3 * broad3 * C3).astype(f32)[:, :1]
        place = lax.broadcasted_iota(jnp.int32, (LINE, 128), 0) // 2
        inside = lax.broadcasted_iota(jnp.int32, (LINE, 128), 0) < 2 * W3
        self.reach = []
        self.col_share = []
        for pc in range(2):
            column = 2 * place + pc
            self.reach.append(jnp.where(inside & (column < line(broad)), line(high), 0))
            edge = (column == 0) | (column == line(broad) - 1)
            self.col_share.append(jnp.where(edge, 0.5, 1.0 / 3.0))
        self.reach3 = jnp.where(inside & (place < line(broad3)), line(self.high3), 0)
        edge3 = (place == 0) | (place == line(broad3) - 1)
        self.col_share3 = jnp.where(edge3, 0.5, 1.0 / 3.0)
        self.flipped = jnp.concatenate([turned] * (STEP // 8), axis=0) > 0

    def share(self, plane, k):
        pr, pc = plane // 2, plane % 2
        return self.lines(4 * k + pr, 2, self.reach[pc], self.col_share[pc], self.high)

    def share3(self, k):
        return self.lines(2 * k, 1, self.reach3, self.col_share3, self.high3)

    def lines(self, row, stride, reach, col_share, height):
        parts = []
        for n in range(2):
            here = row + stride * n
            row_share = jnp.where((here == 0) | (here == height - 1), 0.5, 1.0 / 3.0)
            parts.append(jnp.where(here < reach, line(row_share) * col_share, 0.0))
        return jnp.concatenate(parts, axis=0)


def strip_place(pair, spot, strip_count):
    return lax.rem(pair * 8 + strip_count - 2 + spot, strip_count)


def each_image(bucket_of, pair, visit):
    for image in range(2):
        way = image_shape(bucket_of, pair, image)[2]

        @pl.when(way == 0)
        def _():
            def one(r, carry):
                for plane in range(4):
                    row = 2 * r + plane // 2
                    strip = row // SR
                    there = pl.ds((row - strip * SR) * CW + plane % 2, W3, stride=2)
                    here = pl.ds(r * LINE + image, W3, stride=2)
                    visit(plane, here, image * STRIPS + strip, there)
                return carry

            lax.fori_loop(0, LINES, one, 0)

        @pl.when(way == 1)
        def _():
            def one(r, carry):
                for plane in range(4):
                    for strip in range(STRIPS):
                        first = (plane % 2 + strip * SR) % 2
                        count = (SR - first + 1) // 2
                        done = (strip * SR + first) // 2
                        column = 2 * r + plane // 2
                        there = pl.ds(first * CW + column, count, stride=2 * CW)
                        here = pl.ds(r * LINE + image + 2 * done, count, stride=2)
                        visit(plane, here, image * STRIPS + strip, there)
                return carry

            lax.fori_loop(0, LINES, one, 0)


def row_windows(col_ref, pc, k):
    both = col_ref[pc, step_rows(k, 1)] + col_ref[2 + pc, step_rows(k, 1)]
    return (both + col_ref[2 + pc, step_rows(k)], both + col_ref[pc, step_rows(k, 2)])


def put_col_windows(col_ref, pr, k, even, odd):
    both = even + odd
    col_ref[pr * 2, step_rows(k, 1)] = both + from_left(odd)
    col_ref[pr * 2 + 1, step_rows(k, 1)] = both + from_right(even)


def clear_edges(col_ref):
    zero_line = jnp.zeros((LINE, C2), f32)
    for plane in range(4):
        col_ref[plane, 0:LINE] = zero_line
        col_ref[plane, AREA + LINE : AREA + 2 * LINE] = zero_line


def entry_kernel(pairs, strip_count, piece_count, place_ref, bucket_ref, vec_ref, *refs):
    piece_refs, refs = refs[:piece_count], refs[piece_count:]
    x_out, inv_out, pool_out, mix_out, stat_out, image_ref, col_ref = refs
    pair = pl.program_id(0) if pairs > 1 else 0
    x_ref, inv_ref, pool_ref, mix_ref = (ref.at[0] for ref in (x_out, inv_out, pool_out, mix_out))
    bucket_of = bucket_reader(place_ref, bucket_ref, strip_count)
    shape = Geometry(bucket_of, pair)
    gain1, bias1, scale1 = (vec_ref[n : n + 1] for n in range(3))
    clear_edges(col_ref)
    if piece_count > 1:
        half = piece_count // 2
        for n, ref in enumerate(piece_refs):
            source = place_ref[0] ^ (n // half + 2 * (n % half))
            spot = lax.rem(source + 2, 2 * STRIPS)
            first = 0 if n < half else ref.shape[0] - STRIP_ROWS
            image_ref[spot] = ref[first : first + STRIP_ROWS].astype(f32)
    else:
        for spot in range(2 * STRIPS):
            source = strip_place(pair, spot, strip_count)
            image_ref[spot] = piece_refs[0][source].astype(f32)

    def take_in(plane, here, spot, there):
        x_ref[plane, here] = image_ref[spot, there]

    each_image(bucket_of, pair, take_in)

    def arrange(k, carry):
        total, square = carry
        rows = step_rows(k)
        for plane in range(4):
            share = shape.share(plane, k)
            inv_ref[plane, rows] = share
            values = jnp.where(share > 0.0, x_ref[plane, rows], 0.0)
            x_ref[plane, rows] = values
            total = total + fold(values)
            square = square + fold(values * values)
        return (total, square)

    nothing = jnp.zeros((8, C2), f32)
    total, square = sweep(arrange, (nothing, nothing))
    mean1, scaling1 = norm_terms(total, square, shape.count_two)
    factor1 = scaling1 * gain1
    shift1 = bias1 - mean1 * scaling1 * gain1

    def window_cols(k, carry):
        rows = step_rows(k)
        for pr in range(2):
            masked = []
            for pc in range(2):
                plane = pr * 2 + pc
                normal = rounded(affine(x_ref[plane, rows], factor1, shift1))
                masked.append(jnp.where(inv_ref[plane, rows] > 0.0, normal, 0.0))
            put_col_windows(col_ref, pr, k, *masked)
        return carry

    sweep(window_cols, 0)

    def mix(k, carry):
        total, square = carry
        rows = step_rows(k)
        for pc in range(2):
            windows = row_windows(col_ref, pc, k)
            for pr in range(2):
                plane = pr * 2 + pc
                values = x_ref[plane, rows]
                share = inv_ref[plane, rows]
                pooled = windows[pr] * share - rounded(affine(values, factor1, shift1))
                pooled = jnp.where(share > 0.0, pooled, 0.0)
                mixed = values + scale1 * pooled
                pool_ref[plane, rows] = pooled
                mix_ref[plane, rows] = mixed
                total = total + fold(mixed)
                square = square + fold(mixed * mixed)
        return (total, square)

    total, square = sweep(mix, (nothing, nothing))
    mean2, scaling2 = norm_terms(total, square, shape.count_two)
    for n, value in enumerate((mean1, scaling1, mean2, scaling2)):
        stat_out[0, n] = spread(value, 128)


def pair_specs(pairs, shapes, mode=None):
    if pairs == 1:
        return [VMEM_BLOCK] * len(shapes)
    return [
        pl.BlockSpec(
            (1,) + shape, lambda t, rank=len(shape): (t,) + (0,) * rank, pipeline_mode=mode
        )
        for shape in shapes
    ]


def whole_specs(pairs, shapes):
    if pairs == 1:
        return [VMEM_BLOCK] * len(shapes)
    return [
        pl.BlockSpec(
            shape,
            lambda t, rank=len(shape): (0,) * rank,
            pipeline_mode=pl.Buffered(1),
        )
        for shape in shapes
    ]


def pair_arrays(pairs, shapes, kinds):
    make = pltpu.VMEM if pairs == 1 else jax.ShapeDtypeStruct
    return [make((pairs,) + shape, kind) for shape, kind in zip(shapes, kinds)]


STATE = [(4, AREA, C2)] * 4 + [(4, 8, 128)]
BACK = [(4, AREA, C2)] * 2 + [(2, 8, 128)]


def run_entry(place, buckets, pieces, vec, strip_count):
    pairs = strip_count // 8
    if pairs == 1:
        pieces = held_in(pltpu.VMEM, *pieces)
    return pl.pallas_call(
        functools.partial(entry_kernel, pairs, strip_count, len(pieces)),
        grid=() if pairs == 1 else (pairs,),
        in_specs=[SMEM] * 2 + whole_specs(pairs, [array.shape for array in (vec, *pieces)]),
        out_specs=pair_specs(pairs, STATE),
        out_shape=pair_arrays(pairs, STATE, [f32] * 5),
        scratch_shapes=[
            pltpu.VMEM((2 * STRIPS, STRIP_ROWS, C2), f32),
            pltpu.VMEM((4, AREA + 2 * LINE, C2), f32),
        ],
        compiler_params=roomy(6 if pairs == 1 else 40),
        name="entry",
    )(place, buckets, vec, *pieces)


WEIGHTS = [(C2, HID2), (HID2, C2), (9 * C2, WIDE), (WIDE, HID3), (HID3, WIDE)]


def unpack_kernel(spans, slot_ref, *refs):
    piece_refs, refs = refs[: len(spans)], refs[len(spans) :]
    weights, gathered_ref = refs[:-1], refs[-1]
    done = 0
    for ref, (first, count) in zip(piece_refs, spans):
        blocks = ref[first : first + count * HALF].reshape(count, HALF, 128)
        gathered_ref[done : done + count] = blocks
        done += count
    left_half = lax.broadcasted_iota(jnp.int32, (HALF, 128), 1) < BS
    offset = 0
    for (rows, cols), ref in zip(SHAPES, weights):
        wide = cols // BS
        for rb in range(rows // BS):
            for cb in range(0, wide, 2):
                number = offset + rb * wide + cb
                first = gathered_ref[slot_ref[number]]
                turned = pltpu.roll(first, BS, 1)
                if cb + 1 < wide:
                    second = gathered_ref[slot_ref[number + 1]]
                    top = jnp.where(left_half, first, pltpu.roll(second, BS, 1))
                    low = jnp.where(left_half, turned, second)
                else:
                    top = jnp.where(left_half, first, 0.0)
                    low = jnp.where(left_half, turned, 0.0)
                place = slice(cb * BS, cb * BS + 128)
                ref[rb * BS : rb * BS + HALF, place] = top
                ref[rb * BS + HALF : rb * BS + BS, place] = low
        offset += rows // BS * wide
    weights[3][C3:, :] = jnp.zeros((WIDE - C3, HID3), bf16)


def run_unpack(slot_of, pieces, spans):
    slots = slot_of.shape[0]
    return pl.pallas_call(
        functools.partial(unpack_kernel, spans),
        in_specs=[SMEM] + [VMEM_BLOCK] * len(pieces),
        out_specs=[VMEM_BLOCK] * 5,
        out_shape=[pltpu.VMEM(shape, bf16) for shape in WEIGHTS],
        scratch_shapes=[pltpu.VMEM((slots, HALF, 128), bf16)],
        compiler_params=roomy(6),
        name="unpack",
    )(slot_of, *held_in(pltpu.VMEM, *pieces))


def main_kernel(
    pairs,
    strip_count,
    slots,
    near_place,
    far_place,
    place_ref,
    bucket_ref,
    inv_in,
    mix_in,
    stat_in,
    goal_ref,
    vec_ref,
    w1_ref,
    w2_ref,
    we_ref,
    w3_ref,
    w4_ref,
    result_ref,
    zed_out,
    dx_out,
    mean_out,
    near_ref,
    far_ref,
    flat_ref,
    zed_ref,
    hid_ref,
    u_ref,
    g_ref,
    h_ref,
    dy_ref,
    patch_ref,
    dpatch_ref,
    inv3_ref,
    e_ref,
    col3_ref,
    pool3_ref,
    mix3_ref,
    dx3_ref,
    hid3_ref,
    dhid3_ref,
    u3_ref,
    g3_ref,
    h3_ref,
    dy3_ref,
    dpre_ref,
    gw1_ref,
    gw2_ref,
    gwe_ref,
    gw3_ref,
    gw4_ref,
    acc_two,
    acc_hid_two,
    acc_three,
    acc_hid_three,
):
    pair = pl.program_id(0) if pairs > 1 else 0
    grads = [gw1_ref, gw2_ref, gwe_ref, gw3_ref, gw4_ref]
    inv_ref, mix_ref, stat_ref = (ref.at[0] for ref in (inv_in, mix_in, stat_in))
    back_ref, dx_ref = zed_out.at[0], dx_out.at[0]
    left_half = lax.broadcasted_iota(jnp.int32, (HALF, 128), 1) < BS

    def at_pair(number, act):
        if pairs == 1:
            act()
        else:
            pl.when(pair == number)(act)

    def begin():
        acc_two[...] = jnp.zeros(acc_two.shape, f32)
        acc_hid_two[...] = jnp.zeros(acc_hid_two.shape, f32)
        acc_three[...] = jnp.zeros(acc_three.shape, f32)
        acc_hid_three[...] = jnp.zeros(acc_hid_three.shape, f32)

    at_pair(0, begin)
    shape = Geometry(bucket_reader(place_ref, bucket_ref, strip_count), pair)
    count_two, count_three, flipped = shape.count_two, shape.count_three, shape.flipped
    nothing = jnp.zeros((8, C2), f32)
    nothing3 = jnp.zeros((8, WIDE), f32)

    def vector_row(at, length):
        first, shift = at // 128, at % 128
        count = -(-(shift + length) // 128)
        row = jnp.concatenate([vec_ref[first + n : first + n + 1] for n in range(count)], axis=1)
        if shift:
            row = pltpu.roll(jnp.broadcast_to(row, (8, count * 128)), count * 128 - shift, 1)[:1]
        return row

    def wide_row(at):
        lane = lax.broadcasted_iota(jnp.int32, (1, WIDE), 1)
        return jnp.where(lane < C3, vector_row(at, C3)[:, :WIDE], 0.0)

    gain2, bias2, scale2 = (vec_ref[n : n + 1] for n in range(3, 6))
    hid_bias = vector_row(6 * C2, HID2)
    out_bias = vector_row(6 * C2 + HID2, C2)
    two = 7 * C2 + HID2
    embed_bias, gain3, bias3, scale3 = (wide_row(two + n * C3) for n in range(4))
    gain4, bias4, scale4 = (wide_row(two + n * C3) for n in range(4, 7))
    hid_bias3 = vector_row(two + 7 * C3, HID3)[:, :HID3]
    out_bias3 = wide_row(two + 7 * C3 + HID3)
    mean2, scaling2 = stat_ref[2], stat_ref[3]
    factor2 = scaling2 * gain2
    shift2 = bias2 - mean2 * scaling2 * gain2
    for plane in range(4):
        zed_ref[plane, 0:LINE] = jnp.zeros((LINE, C2), f32)
    col3_ref[0:LINE] = jnp.zeros((LINE, WIDE), f32)
    col3_ref[AREA + LINE : AREA + 2 * LINE] = jnp.zeros((LINE, WIDE), f32)

    def put_block(number, block):
        near_ref[near_place[number]] = block
        far_ref[far_place[number]] = block

    def pack_blocks(matrices):
        offsets = [0]
        for rows, cols in SHAPES:
            offsets.append(offsets[-1] + rows // BS * (cols // BS))
        for which in matrices:
            (rows, cols), ref = SHAPES[which], grads[which]
            wide = cols // BS
            for rb in range(rows // BS):
                for cb in range(0, wide, 2):
                    number = offsets[which] + rb * wide + cb
                    at = slice(cb * BS, cb * BS + 128)
                    top = ref[rb * BS : rb * BS + HALF, at].astype(bf16)
                    low = ref[rb * BS + HALF : rb * BS + BS, at].astype(bf16)
                    put_block(number, jnp.where(left_half, top, pltpu.roll(low, BS, 1)))
                    if cb + 1 < wide:
                        put_block(number + 1, jnp.where(left_half, pltpu.roll(top, BS, 1), low))

    def plane_rows(plane):
        return slice(plane * AREA, plane * AREA + AREA)

    def begin_plane(plane):
        low = affine(mix_ref[plane], factor2, shift2).astype(bf16)
        h_ref[plane_rows(plane)] = low
        hid_ref[plane % 2] = product(low, w1_ref[...])

    begin_plane(0)
    for plane in range(4):
        if plane < 3:
            begin_plane(plane + 1)
        for k in range(STEPS):
            rows = step_rows(k)
            flat = slice(plane * AREA + k * STEP, plane * AREA + k * STEP + STEP)
            for at in range(0, HID2, 128):
                lanes = slice(at, at + 128)
                active, slope = gelu_pair(hid_ref[plane % 2, rows, lanes] + hid_bias[:, lanes])
                u_ref[flat, lanes] = active.astype(bf16)
                g_ref[flat, lanes] = slope.astype(bf16)
        out = product(u_ref[plane_rows(plane)], w2_ref[...]) + out_bias
        zed = jnp.where(inv_ref[plane] > 0.0, mix_ref[plane] + scale2 * out, 0.0)
        zed_ref[plane, LINE : LINE + AREA] = rounded(zed)

    def patches(k, carry):
        rows = step_rows(k)
        taps = []
        for ky in range(3):
            pr = (0 if ky == 1 else 1) * 2
            source = step_rows(k, 0 if ky == 0 else 1)
            even = zed_ref[pr, source]
            odd = zed_ref[pr + 1, source]
            taps.append((from_left(odd), even, odd))
        for ky in range(3):
            for kx in range(3):
                at = (3 * ky + kx) * C2
                tap = taps[ky][kx]
                if ky != kx:
                    tap = jnp.where(flipped, taps[kx][ky], tap)
                patch_ref[rows, at : at + C2] = tap.astype(bf16)
        return carry

    sweep(patches, 0)
    e_ref[...] = product(patch_ref[...], we_ref[...])

    def embed(k, carry):
        total, square = carry
        rows = step_rows(k)
        share = shape.share3(k)
        inv3_ref[rows] = share
        out = jnp.where(widen(share) > 0.0, e_ref[rows] + embed_bias, 0.0)
        e_ref[rows] = out
        return (total + fold(out), square + fold(out * out))

    total, square = sweep(embed, (nothing3, nothing3))
    mean3, scaling3 = norm_terms(total, square, count_three)
    factor3 = scaling3 * gain3
    shift3 = bias3 - mean3 * scaling3 * gain3

    def window_cols3(k, carry):
        rows = step_rows(k)
        normal = rounded(affine(e_ref[rows], factor3, shift3))
        masked = jnp.where(widen(inv3_ref[rows]) > 0.0, normal, 0.0)
        col3_ref[step_rows(k, 1)] = masked + from_left(masked) + from_right(masked)
        return carry

    sweep(window_cols3, 0)

    def row_windows3(k):
        return col3_ref[step_rows(k)] + col3_ref[step_rows(k, 1)] + col3_ref[step_rows(k, 2)]

    def mix3(k, carry):
        total, square = carry
        rows = step_rows(k)
        values = e_ref[rows]
        share = widen(inv3_ref[rows])
        pooled = row_windows3(k) * share - rounded(affine(values, factor3, shift3))
        pooled = jnp.where(share > 0.0, pooled, 0.0)
        mixed = values + scale3 * pooled
        pool3_ref[rows] = pooled
        mix3_ref[rows] = mixed
        return (total + fold(mixed), square + fold(mixed * mixed))

    total, square = sweep(mix3, (nothing3, nothing3))
    mean4, scaling4 = norm_terms(total, square, count_three)
    factor4 = scaling4 * gain4
    shift4 = bias4 - mean4 * scaling4 * gain4
    normal4 = (spread(scaling4, WIDE), spread(-mean4 * scaling4, WIDE))

    def prepare3(k, d_bias):
        rows = step_rows(k)
        h3_ref[rows] = affine(mix3_ref[rows], factor4, shift4).astype(bf16)
        goal = goal_ref[0, rows].astype(f32)
        goal = jnp.where(widen(inv3_ref[rows]) > 0.0, goal, 0.0)
        goal = scale4 * goal
        dy3_ref[rows] = goal.astype(bf16)
        return d_bias + fold(goal)

    acc_three[7] += sweep(prepare3, nothing3)

    def keep(ref, value, place=slice(None)):
        if pairs == 1:
            ref[place] = value.astype(ref.dtype)
        else:

            @pl.when(pair == 0)
            def _():
                ref[place] = value

            @pl.when(pair > 0)
            def _():
                ref[place] += value

    def begin_chunk(at):
        lanes = slice(at, at + 256)
        hid3_ref[:, lanes] = product(h3_ref[...], w3_ref[:, lanes])
        dhid3_ref[:, lanes] = product_nt(dy3_ref[...], w4_ref[lanes])

    begin_chunk(0)
    for at in range(0, HID3, 256):
        if at + 256 < HID3:
            begin_chunk(at + 256)
        for lane in (at, at + 128):
            lanes = slice(lane, lane + 128)
            total = nothing
            for k in range(STEPS):
                rows = step_rows(k)
                active, slope = gelu_pair(hid3_ref[rows, lanes] + hid_bias3[:, lanes])
                u3_ref[rows, lanes] = active.astype(bf16)
                change = slope * dhid3_ref[rows, lanes]
                g3_ref[rows, lanes] = change.astype(bf16)
                total = total + fold(change)
            acc_hid_three[:, lanes] += total
        lanes = slice(at, at + 256)
        out = product(u3_ref[:, lanes], w4_ref[lanes])
        d_low = product_nt(g3_ref[:, lanes], w3_ref[:, lanes])
        result_ref[0] = out if at == 0 else result_ref[0] + out
        dx3_ref[...] = d_low if at == 0 else dx3_ref[...] + d_low
        keep(gw3_ref, product_tn(h3_ref[...], g3_ref[:, lanes]), (slice(None), lanes))
        keep(gw4_ref, product_tn(u3_ref[:, lanes], dy3_ref[...]), lanes)

    def finish3(k, carry):
        d_scale, d_shift, d_gain = carry
        rows = step_rows(k)
        valid = widen(inv3_ref[rows]) > 0.0
        mixed = mix3_ref[rows]
        out = jnp.where(valid, result_ref[0, rows] + out_bias3, 0.0)
        result_ref[0, rows] = mixed + scale4 * out
        d_scale = d_scale + fold(out * goal_ref[0, rows].astype(f32))
        d_low = dx3_ref[rows]
        normal = affine(mixed, *normal4)
        return (d_scale, d_shift + fold(d_low), d_gain + fold(d_low * normal))

    d_scale, d_shift, d_gain = sweep(finish3, (nothing3, nothing3, nothing3))
    acc_three[6] += d_scale
    acc_three[5] += d_shift
    acc_three[4] += d_gain
    mean_shift = by_image(d_shift * gain4) / count_three
    mean_gain = by_image(d_gain * gain4) / count_three
    back_gain4 = scaling4 * gain4
    back_mean4 = spread(-scaling4 * mean_shift, WIDE)
    back_normal4 = spread(scaling4 * mean_gain, WIDE)

    def unmix3(k, d_scale):
        rows = step_rows(k)
        share = widen(inv3_ref[rows])
        valid = share > 0.0
        normal = affine(mix3_ref[rows], *normal4)
        back = affine(dx3_ref[rows], back_gain4, back_mean4) - scaled(normal, back_normal4)
        d_mixed = jnp.where(valid, back + goal_ref[0, rows].astype(f32), 0.0)
        dx3_ref[rows] = d_mixed
        d_scale = d_scale + fold(pool3_ref[rows] * d_mixed)
        weighted = scale3 * d_mixed * share
        col3_ref[step_rows(k, 1)] = weighted + from_left(weighted) + from_right(weighted)
        return d_scale

    acc_three[3] += sweep(unmix3, nothing3)
    normal3 = (spread(scaling3, WIDE), spread(-mean3 * scaling3, WIDE))

    def unpool3(k, carry):
        d_shift, d_gain = carry
        rows = step_rows(k)
        valid = widen(inv3_ref[rows]) > 0.0
        d_normal = jnp.where(valid, row_windows3(k) - scale3 * dx3_ref[rows], 0.0)
        pool3_ref[rows] = d_normal
        normal = affine(e_ref[rows], *normal3)
        return (d_shift + fold(d_normal), d_gain + fold(d_normal * normal))

    d_shift, d_gain = sweep(unpool3, (nothing3, nothing3))
    acc_three[2] += d_shift
    acc_three[1] += d_gain
    mean_shift = by_image(d_shift * gain3) / count_three
    mean_gain = by_image(d_gain * gain3) / count_three
    back_gain3 = scaling3 * gain3
    back_mean3 = spread(-scaling3 * mean_shift, WIDE)
    back_normal3 = spread(scaling3 * mean_gain, WIDE)

    def unnorm3(k, d_bias):
        rows = step_rows(k)
        valid = widen(inv3_ref[rows]) > 0.0
        normal = affine(e_ref[rows], *normal3)
        back = affine(pool3_ref[rows], back_gain3, back_mean3) - scaled(normal, back_normal3)
        low = jnp.where(valid, dx3_ref[rows] + back, 0.0).astype(bf16)
        dpre_ref[rows] = low
        return d_bias + fold(low.astype(f32))

    acc_three[0] += sweep(unnorm3, nothing3)
    keep(gwe_ref, product_tn(patch_ref[...], dpre_ref[...]))
    dpatch_ref[0:AREA] = product_nt(dpre_ref[...], we_ref[...])
    dpatch_ref[AREA : AREA + LINE] = jnp.zeros((LINE, 9 * C2), f32)

    def gather_back(k, carry):
        rows = step_rows(k)

        def tap(ky, kx, source):
            at = (3 * ky + kx) * C2
            value = dpatch_ref[source, at : at + C2]
            if ky != kx:
                at = (3 * kx + ky) * C2
                value = jnp.where(flipped, dpatch_ref[source, at : at + C2], value)
            return value

        sources = []
        for ky in range(3):
            source = step_rows(k, 1 if ky == 0 else 0)
            sources.append(
                (tap(ky, 1, source), tap(ky, 2, source) + from_right(tap(ky, 0, source)))
            )
        for pc in range(2):
            for pr, value in ((0, sources[1][pc]), (1, sources[2][pc] + sources[0][pc])):
                plane = pr * 2 + pc
                valid = inv_ref[plane, rows] > 0.0
                back_ref[plane, rows] = jnp.where(valid, rounded(value), 0.0)
        return carry

    sweep(gather_back, 0)

    if pairs == 1:
        pack_blocks(range(2, 5))

    normal2 = (spread(scaling2, C2), spread(-mean2 * scaling2, C2))

    def begin_back(plane):
        goal = scale2 * back_ref[plane]
        dy_ref[plane_rows(plane)] = goal.astype(bf16)
        hid_ref[plane % 2] = product_nt(goal.astype(bf16), w2_ref[...])
        return fold(goal)

    d_out_bias = begin_back(0)
    d_shift, d_gain = nothing, nothing
    sums = [nothing] * (HID2 // 128)
    new_gw1, new_gw2 = None, None
    for plane in range(4):
        if plane < 3:
            d_out_bias = d_out_bias + begin_back(plane + 1)
        for k in range(STEPS):
            rows = step_rows(k)
            part = slice(plane * AREA + k * STEP, plane * AREA + k * STEP + STEP)
            for n, at in enumerate(range(0, HID2, 128)):
                lanes = slice(at, at + 128)
                change = g_ref[part, lanes].astype(f32) * hid_ref[plane % 2, rows, lanes]
                g_ref[part, lanes] = change.astype(bf16)
                sums[n] = sums[n] + fold(change)
        flat = plane_rows(plane)
        d_low = product_nt(g_ref[flat], w1_ref[...])
        dx_ref[plane] = d_low
        d_shift = d_shift + fold(d_low)
        d_gain = d_gain + fold(d_low * affine(mix_ref[plane], *normal2))
        part_gw1 = product_tn(h_ref[flat], g_ref[flat])
        part_gw2 = product_tn(dy_ref[flat], u_ref[flat])
        new_gw1 = part_gw1 if plane == 0 else new_gw1 + part_gw1
        new_gw2 = part_gw2 if plane == 0 else new_gw2 + part_gw2
    new_gw2 = new_gw2.T
    for n, value in enumerate(sums):
        acc_hid_two[:, n * 128 : n * 128 + 128] += value
    acc_two[6] += d_out_bias
    acc_two[4] += d_shift
    acc_two[3] += d_gain
    mean_out[0, 0] = spread(by_image(d_shift * gain2) / count_two, 128)
    mean_out[0, 1] = spread(by_image(d_gain * gain2) / count_two, 128)
    keep(gw1_ref, new_gw1)
    keep(gw2_ref, new_gw2)
    d_scale = fold(w2_ref[...].astype(f32) * new_gw2) + out_bias * d_out_bias
    acc_two[5] += d_scale / scale2

    def finish():
        if pairs > 1:
            pack_blocks(range(5))
        else:
            pack_blocks(range(2))

        def filler(number, carry):
            put_block(number, jnp.zeros((HALF, 128), bf16))
            return carry

        lax.fori_loop(USED, slots, filler, 0)

        flat_ref[...] = jnp.zeros(flat_ref.shape, f32)

        def put(at, total, length):
            if at % 128:
                room = jnp.zeros((8, 128), f32)
                if total.shape[1] < length + BS:
                    total = jnp.concatenate([total, room], axis=1)
                total = pltpu.roll(total, BS, 1)
            whole = jnp.sum(total, axis=0, keepdims=True)
            done = -(at % 128)
            row = at // 128
            lane = 0
            while done < length:
                first = max(0, -done)
                last = min(128, length - done)
                flat_ref[row : row + 1, first:last] = whole[:, lane + first : lane + last]
                done += 128
                lane += 128
                row += 1

        at = 3 * C2
        for n in range(3, 6):
            put(at, acc_two[n], C2)
            at += C2
        put(at, acc_hid_two[...], HID2)
        at += HID2
        put(at, acc_two[6], C2)
        at += C2
        for n in range(7):
            put(at, acc_three[n], C3)
            at += C3
        put(at, acc_hid_three[...], HID3)
        at += HID3
        put(at, acc_three[7], C3)

    at_pair(pairs - 1, finish)


def run_main(places, place, buckets, state, goal, vec, weights, strip_count):
    pairs = goal.shape[0]
    slots = places[0].shape[0]
    half = slots // 2 + 1
    if pairs == 1:
        state = held_in(pltpu.VMEM, *state)
    weights = held_in(pltpu.VMEM, *weights)
    _, inv, _, mix, stat = state
    state_shapes = [STATE[1], STATE[3], STATE[4]]
    grad_kind = bf16 if pairs == 1 else f32
    wide_f32 = pltpu.VMEM((AREA, WIDE), f32)
    wide_bf16 = pltpu.VMEM((AREA, WIDE), bf16)
    scratch = [
        pltpu.VMEM((4, AREA + LINE, C2), f32),
        pltpu.VMEM((2, AREA, HID2), f32),
        pltpu.VMEM((4 * AREA, HID2), bf16),
        pltpu.VMEM((4 * AREA, HID2), bf16),
        pltpu.VMEM((4 * AREA, C2), bf16),
        pltpu.VMEM((4 * AREA, C2), bf16),
        pltpu.VMEM((AREA, 9 * C2), bf16),
        pltpu.VMEM((AREA + LINE, 9 * C2), f32),
        pltpu.VMEM((AREA, 128), f32),
        wide_f32,
        pltpu.VMEM((AREA + 2 * LINE, WIDE), f32),
        wide_f32,
        wide_f32,
        wide_f32,
        pltpu.VMEM((AREA, HID3), f32),
        pltpu.VMEM((AREA, HID3), f32),
        pltpu.VMEM((AREA, HID3), bf16),
        pltpu.VMEM((AREA, HID3), bf16),
        wide_bf16,
        wide_bf16,
        wide_bf16,
        pltpu.VMEM((C2, HID2), grad_kind),
        pltpu.VMEM((HID2, C2), grad_kind),
        pltpu.VMEM((9 * C2, WIDE), grad_kind),
        pltpu.VMEM((WIDE, HID3), grad_kind),
        pltpu.VMEM((HID3, WIDE), grad_kind),
        pltpu.VMEM((7, 8, C2), f32),
        pltpu.VMEM((8, HID2), f32),
        pltpu.VMEM((8, 8, WIDE), f32),
        pltpu.VMEM((8, HID3), f32),
    ]
    out_shapes = [(half, HALF, 128), (half, HALF, 128), (VEC_BLOCKS * HALF, 128)]
    make = pltpu.VMEM if pairs == 1 else jax.ShapeDtypeStruct
    return pl.pallas_call(
        functools.partial(main_kernel, pairs, strip_count, slots),
        grid=() if pairs == 1 else (pairs,),
        in_specs=[SMEM] * 4
        + pair_specs(pairs, state_shapes + [goal.shape[1:]], pl.Buffered(1))
        + whole_specs(pairs, [vec.shape])
        + [VMEM_BLOCK] * 5,
        out_specs=pair_specs(pairs, [(AREA, WIDE)] + BACK) + whole_specs(pairs, out_shapes),
        out_shape=pair_arrays(pairs, [(AREA, WIDE)] + BACK, [f32] * 4)
        + [make(shape, kind) for shape, kind in zip(out_shapes, (bf16, bf16, f32))],
        scratch_shapes=scratch,
        compiler_params=pltpu.CompilerParams(
            vmem_limit_bytes=(40 if pairs == 1 else 56) * 1024 * 1024,
        ),
        name="blocks",
    )(*places, place, buckets, inv, mix, stat, goal, vec, *weights)


def exit_kernel(
    pairs,
    strip_count,
    place_ref,
    bucket_ref,
    x_in,
    inv_in,
    pool_in,
    mix_in,
    stat_in,
    zed_in,
    dx_in,
    mean_in,
    flat_ref,
    vec_ref,
    payload_hbm,
    vector_ref,
    payload_ref,
    image_ref,
    col_ref,
    dx_ref,
    back_ref,
    acc_ref,
    sem,
):
    pair = pl.program_id(0) if pairs > 1 else 0
    x_ref, inv_ref, pool_ref, mix_ref, stat_ref, zed_ref, low_ref, mean_ref = (
        ref.at[0] for ref in (x_in, inv_in, pool_in, mix_in, stat_in, zed_in, dx_in, mean_in)
    )
    bucket_of = bucket_reader(place_ref, bucket_ref, strip_count)
    shape = Geometry(bucket_of, pair)
    count_two = shape.count_two
    gain1, bias1, scale1, gain2 = (vec_ref[n : n + 1] for n in range(4))
    mean1, scaling1, mean2, scaling2 = (stat_ref[n] for n in range(4))
    normal2 = (scaling2, -mean2 * scaling2)
    clear_edges(col_ref)
    nothing = jnp.zeros((8, C2), f32)
    back_gain2 = scaling2 * gain2
    back_mean2 = -scaling2 * mean_ref[0]
    back_normal2 = scaling2 * mean_ref[1]

    if pairs > 1:

        @pl.when(pair == 0)
        def _():
            acc_ref[...] = jnp.zeros(acc_ref.shape, f32)

    def add_up(n, total):
        acc_ref[n] = total if pairs == 1 else acc_ref[n] + total

    def unmix(k, d_scale):
        rows = step_rows(k)
        for pr in range(2):
            weighted = []
            for pc in range(2):
                plane = pr * 2 + pc
                share = inv_ref[plane, rows]
                normal = affine(mix_ref[plane, rows], *normal2)
                back = affine(low_ref[plane, rows], back_gain2, back_mean2)
                back = back - scaled(normal, back_normal2)
                d_mixed = jnp.where(share > 0.0, zed_ref[plane, rows] + back, 0.0)
                dx_ref[plane, rows] = d_mixed
                d_scale = d_scale + fold(pool_ref[plane, rows] * d_mixed)
                weighted.append(scale1 * d_mixed * share)
            put_col_windows(col_ref, pr, k, *weighted)
        return d_scale

    add_up(2, sweep(unmix, nothing))
    normal1 = (spread(scaling1, C2), spread(-mean1 * scaling1, C2))

    def unpool(k, carry):
        d_shift, d_gain = carry
        rows = step_rows(k)
        for pc in range(2):
            windows = row_windows(col_ref, pc, k)
            for pr in range(2):
                plane = pr * 2 + pc
                valid = inv_ref[plane, rows] > 0.0
                d_normal = windows[pr] - scale1 * dx_ref[plane, rows]
                d_normal = jnp.where(valid, d_normal, 0.0)
                back_ref[plane, rows] = d_normal
                normal = affine(x_ref[plane, rows], *normal1)
                d_shift = d_shift + fold(d_normal)
                d_gain = d_gain + fold(d_normal * normal)
        return (d_shift, d_gain)

    d_shift, d_gain = sweep(unpool, (nothing, nothing))
    add_up(1, d_shift)
    add_up(0, d_gain)
    mean_shift = by_image(d_shift * gain1) / count_two
    mean_gain = by_image(d_gain * gain1) / count_two
    back_gain1 = scaling1 * gain1
    back_mean1 = spread(-scaling1 * mean_shift, C2)
    back_normal1 = spread(scaling1 * mean_gain, C2)

    def unnorm(k, carry):
        rows = step_rows(k)
        for plane in range(4):
            normal = affine(x_ref[plane, rows], *normal1)
            back = affine(back_ref[plane, rows], back_gain1, back_mean1)
            back = back - scaled(normal, back_normal1)
            valid = inv_ref[plane, rows] > 0.0
            dx_ref[plane, rows] = jnp.where(valid, dx_ref[plane, rows] + back, 0.0)
        return carry

    sweep(unnorm, 0)

    def give_back(plane, here, spot, there):
        image_ref[spot, there] = dx_ref[plane, here]

    image_ref[...] = jnp.zeros(image_ref.shape, f32)
    each_image(bucket_of, pair, give_back)

    for spot in range(2 * STRIPS):
        target = strip_place(pair, spot, strip_count)
        for within in range(SR):
            rows = slice(within * CW, within * CW + CW)
            payload_ref[target, within] = image_ref[spot, rows].astype(bf16)

    def finish():
        copy = pltpu.make_async_copy(payload_ref, payload_hbm, sem)
        copy.start()
        vector_ref[...] = flat_ref[...]
        for n in range(3):
            vector_ref[n : n + 1] = jnp.sum(acc_ref[n], axis=0, keepdims=True)
        copy.wait()

    if pairs == 1:
        finish()
    else:
        pl.when(pair == pairs - 1)(finish)


def run_exit(place, buckets, state, back, flat, vec, strip_count):
    pairs = strip_count // 8
    payload = (strip_count, SR, CW, C2)
    make = pltpu.VMEM if pairs == 1 else jax.ShapeDtypeStruct
    plane_f32 = pltpu.VMEM((4, AREA, C2), f32)
    arrays = [*state, *back]
    if pairs == 1:
        arrays = held_in(pltpu.VMEM, *arrays)
    return pl.pallas_call(
        functools.partial(exit_kernel, pairs, strip_count),
        grid=() if pairs == 1 else (pairs,),
        in_specs=[SMEM] * 2
        + pair_specs(pairs, STATE + BACK, pl.Buffered(1))
        + whole_specs(pairs, [flat.shape, vec.shape]),
        out_specs=[HBM] + whole_specs(pairs, [flat.shape]),
        out_shape=[pltpu.HBM(payload, bf16), make(flat.shape, f32)],
        scratch_shapes=[
            pltpu.VMEM(payload, bf16),
            pltpu.VMEM((2 * STRIPS, STRIP_ROWS, C2), f32),
            pltpu.VMEM((4, AREA + 2 * LINE, C2), f32),
            plane_f32,
            plane_f32,
            pltpu.VMEM((3, 8, C2), f32),
            pltpu.SemaphoreType.DMA,
        ],
        compiler_params=roomy(8 if pairs == 1 else 40),
        name="exit",
    )(place, buckets, *arrays, flat, vec)


def dense_blocks(values):
    return jnp.concatenate([values[:, :HALF], values[:, HALF:]], axis=2).astype(bf16)


def pack_kernel(master_ref, dense_ref):
    dense_ref[...] = dense_blocks(master_ref[...])


def pack(master):
    owned = master.shape[0]
    return pl.pallas_call(
        pack_kernel,
        out_shape=jax.ShapeDtypeStruct((owned, HALF, 2 * BS), bf16),
        name="pack",
    )(master)


def pack_pieces_kernel(place_ref, master_hbm, pixel_hbm, *refs):
    out_refs, (wide_ref, master_ref, pixel_ref, sem) = refs[:-4], refs[-4:]
    owned = master_ref.shape[0]
    slots = pixel_ref.shape[2]
    copies = [pltpu.make_async_copy(pixel_hbm, pixel_ref, sem.at[0])]
    parts = [(0, owned // 2), (owned // 2, owned - owned // 2)]
    for n, part in enumerate(parts):
        copies.append(
            pltpu.make_async_copy(
                master_hbm.at[pl.ds(*part)], master_ref.at[pl.ds(*part)], sem.at[1 + n]
            )
        )
    for copy in copies:
        copy.start()
    copies[0].wait()

    def widen_row(row, carry):
        start = pl.multiple_of(row * CW * slots, 8)
        values = pixel_ref[row].astype(f32).reshape(CW * slots, C2)
        wide_ref[pl.ds(start, CW * slots)] = values
        return carry

    lax.fori_loop(0, SR, widen_row, 0)
    for k, ref in enumerate(out_refs):
        for other in range(2):
            slot = place_ref[0] ^ (2 * k + other)
            first = other * (ref.shape[0] - STRIP_ROWS)
            strip = wide_ref[pl.ds(slot, STRIP_ROWS, stride=slots)]
            ref[first : first + STRIP_ROWS] = strip.astype(bf16)
    for (first, count), copy in zip(parts, copies[1:]):
        copy.wait()
        dense = dense_blocks(master_ref[first : first + count]).reshape(count * HALF, 2 * BS)
        start = STRIP_ROWS + first * HALF
        for ref in out_refs[:3]:
            ref[start : start + count * HALF] = dense


def pack_pieces(place, master, pixels):
    slots = pixels.shape[2]
    rows = master.shape[0] * HALF
    shapes = [(rows + 2 * STRIP_ROWS, 2 * BS)] * 3 + [(2 * STRIP_ROWS, 2 * BS)]
    return pl.pallas_call(
        pack_pieces_kernel,
        in_specs=[SMEM] + [HBM] * 2,
        out_specs=[VMEM_BLOCK] * 4,
        out_shape=[pltpu.VMEM(shape, bf16) for shape in shapes],
        scratch_shapes=[
            pltpu.VMEM((STRIP_ROWS * slots, C2), f32),
            pltpu.VMEM(master.shape, f32),
            pltpu.VMEM(pixels.shape, bf16),
            pltpu.SemaphoreType.DMA((3,)),
        ],
        compiler_params=roomy(12),
        name="pack",
    )(place, *held_in(pltpu.HBM, master, pixels))


def fold_pair_kernel(near_ref, got_ref, own_ref, *part_refs):
    share = own_ref.shape[0]

    def one(n, carry):
        own_ref[n] = near_ref[n].astype(f32) + got_ref[n].astype(f32)
        for k, ref in enumerate(part_refs):
            here = (k + 1) * share + n
            ref[n] = near_ref[here] + got_ref[here]
        return carry

    lax.fori_loop(0, share, one, 0, unroll=4)


def fold_pair(near, got, groups):
    shape = ((near.shape[0] - 1) // groups,) + near.shape[1:]
    return pl.pallas_call(
        fold_pair_kernel,
        in_specs=[VMEM_BLOCK] * 2,
        out_specs=[VMEM_BLOCK] * groups,
        out_shape=[pltpu.VMEM(shape, f32)] + [pltpu.VMEM(shape, bf16)] * (groups - 1),
        compiler_params=roomy(4),
        name="fold_pair",
    )(*held_in(pltpu.VMEM, near, got))


def fold_tile_kernel(pieces, spot_ref, *refs):
    piece_refs, refs = refs[:pieces], refs[pieces:]
    vector_refs, refs = refs[:pieces], refs[pieces:]
    out_refs, sum_ref = refs[:-1], refs[-1]
    groups = len(out_refs)
    share = out_refs[0].shape[0]
    owned = piece_refs[0].shape[0]
    total = vector_refs[0][...]
    for ref in vector_refs[1:]:
        total = total + ref[...]
    for n in range(sum_ref.shape[0]):
        sum_ref[n] = jnp.zeros((HALF, 128), f32)
    for n in range(VEC_BLOCKS):
        sum_ref[n] = total[n * HALF : (n + 1) * HALF]

    def one(n, carry):
        for k, out_ref in enumerate(out_refs):
            number = lax.rem(spot_ref[0] + k, groups) * share + n
            block = jnp.minimum(number, owned - 1)
            total = piece_refs[0][block].astype(f32)
            for ref in piece_refs[1:]:
                total = total + ref[block].astype(f32)
            rest = sum_ref[jnp.maximum(number - owned, 0)]
            out_ref[n] = jnp.where(number < owned, total, rest).astype(out_ref.dtype)
        return carry

    lax.fori_loop(0, share, one, 0, unroll=share <= 16)


def fold_tile(spot, pieces, vectors, extra, groups):
    shape = ((pieces[0].shape[0] + extra) // groups,) + pieces[0].shape[1:]
    return pl.pallas_call(
        functools.partial(fold_tile_kernel, len(pieces)),
        in_specs=[SMEM] + [VMEM_BLOCK] * (len(pieces) + len(vectors)),
        out_specs=[VMEM_BLOCK] * groups,
        out_shape=[pltpu.VMEM(shape, f32)] + [pltpu.VMEM(shape, bf16)] * (groups - 1),
        scratch_shapes=[pltpu.VMEM((extra, HALF, 128), f32)],
        compiler_params=roomy(8),
        name="fold_tile",
    )(spot, *held_in(pltpu.VMEM, *pieces, *vectors))


def fold_batch_kernel(owned, vector_weight, spot_ref, *refs):
    part_refs, (total_ref, norm_ref) = refs[:-2], refs[-2:]
    share = total_ref.shape[0]
    square = jnp.zeros((8, 128), f32)
    for n in range(share):
        total = part_refs[0][n].astype(f32)
        for ref in part_refs[1:]:
            total = total + ref[n].astype(f32)
        total_ref[n] = total.astype(bf16)
        weight = jnp.where(spot_ref[0] * share + n < owned, 1.0, vector_weight)
        square = square + weight * fold(total * total)
    square = jnp.sum(jnp.sum(square, axis=1, keepdims=True), axis=0, keepdims=True)
    norm_ref[...] = jnp.broadcast_to(square[None], norm_ref.shape)


def fold_batch(spot, parts, owned, tile_count):
    count = tile_count * len(parts)
    return pl.pallas_call(
        functools.partial(fold_batch_kernel, owned, 1.0 / tile_count),
        in_specs=[SMEM] + [VMEM_BLOCK] * len(parts),
        out_specs=[VMEM_BLOCK] * 2,
        out_shape=[pltpu.VMEM(parts[0].shape, bf16), pltpu.VMEM((count, 1, 128), f32)],
        name="fold_batch",
    )(spot, *held_in(pltpu.VMEM, *parts))


def update_kernel(owned, groups, spot_ref, norm_ref, *refs):
    quarters, refs = refs[:groups], refs[groups:]
    stat_hbm, out_hbm, (vector_ref, clip_ref), refs = refs[:5], refs[5:10], refs[10:12], refs[12:]
    stat_refs, out_refs, (in_sem, out_sem) = refs[:5], refs[5:10], refs[10:]
    master_ref, left_stat_ref, right_stat_ref, left_root_ref, right_root_ref = stat_refs
    grad_ref, left_ref, right_ref, new_ref, copy_ref = out_refs
    share = quarters[0].shape[0]
    spans = spans_of(owned)

    def copies_of(sources, targets, sems):
        return [
            [
                pltpu.make_async_copy(
                    source.at[pl.ds(*span)], target.at[pl.ds(*span)], sems.at[5 * n + k]
                )
                for k, (source, target) in enumerate(zip(sources, targets))
            ]
            for n, span in enumerate(spans)
        ]

    copies_in = copies_of(stat_hbm, stat_refs, in_sem)
    copies_out = copies_of(out_refs, out_hbm, out_sem)
    for copies in copies_in:
        for copy in copies:
            copy.start()
    norm = jnp.sqrt(jnp.sum(norm_ref[...], axis=0))
    factor = jnp.minimum(1.0, clip_limit / norm)
    left_half = lax.broadcasted_iota(jnp.int32, (HALF, 128), 1) < BS

    def summed(number):
        source = number // share
        local = number - source * share
        turn = lax.rem(spot_ref[0] - source + groups, groups)
        value = quarters[0][local].astype(f32)
        for k in range(1, groups):
            value = jnp.where(turn == k, quarters[k][local].astype(f32), value)
        return value * factor

    def side_by_side(first, count):
        sides = []
        for n in range(first, first + count, 2):
            dense = summed(n)
            turned = pltpu.roll(dense, BS, 1)
            if n + 1 < first + count:
                second = summed(n + 1)
                top = jnp.where(left_half, dense, pltpu.roll(second, BS, 1))
                low = jnp.where(left_half, turned, second)
                side = jnp.concatenate([top, low], axis=0)
                grad_ref[n + 1] = pltpu.roll(side, BS, 1)[:, :BS]
            else:
                side = jnp.concatenate([dense, turned], axis=0)[:, :BS]
            grad_ref[n] = side[:, :BS]
            sides.append(side.astype(bf16))
        return jnp.concatenate(sides, axis=1)

    def diagonal_of(count):
        order = (count * BS, count * BS)
        return lax.broadcasted_iota(jnp.int32, order, 0) // BS == (
            lax.broadcasted_iota(jnp.int32, order, 1) // BS
        )

    clip_ref[...] = norm
    for n in range(vector_ref.shape[0]):
        vector_ref[n] = summed(owned + n)
    for (first, length), arriving, leaving in zip(spans, copies_in, copies_out):
        parts = [(n, min(4, first + length - n)) for n in range(first, first + length, 4)]
        wides = [side_by_side(*part) for part in parts]
        tall = [
            jnp.where(diagonal_of(count), jnp.concatenate([wide] * count, axis=0), 0.0)
            for (_, count), wide in zip(parts, wides)
        ]
        lefts = [product_nt(one, wide) for one, wide in zip(tall, wides)]
        rights = [product_tn(wide, wide) for wide in wides]
        for copy in arriving:
            copy.wait()
        stepped = []
        for (start, count), wide in zip(parts, wides):
            roots = left_root_ref[pl.ds(start, count)].reshape(count * BS, BS).astype(bf16)
            stepped.append(product(roots, wide))
        for (start, count), left, right in zip(parts, lefts, rights):
            here = pl.ds(start, count)
            left_ref[here] = 0.5 * left_stat_ref[here] + 0.5 * left.reshape(count, BS, BS)
            for n in range(count):
                at = n // 2 * 128
                block = right[n * BS : n * BS + BS, at : min(at + 128, count * BS)]
                if n % 2:
                    block = pltpu.roll(block, BS, 1)
                right_ref[start + n] = 0.5 * right_stat_ref[start + n] + 0.5 * block[:, :BS]
        for (start, count), value in zip(parts, stepped):
            here = pl.ds(start, count)
            value = jnp.where(diagonal_of(count), value, 0.0).astype(bf16)
            roots = right_root_ref[here].reshape(count * BS, BS).astype(bf16)
            value = product(value, roots).reshape(count, BS, BS)
            new = master_ref[here] - rate_matrix * value
            new_ref[here] = new
            copy_ref[here] = new.astype(bf16)
        for copy in leaving:
            copy.start()
    for leaving in copies_out:
        for copy in leaving:
            copy.wait()


def spans_of(owned):
    spans = []
    first = 0
    while first < owned:
        length = min(8 if first == 0 else 12, owned - first)
        spans.append((first, length))
        first += length
    return spans


def update(spot, norm, quarters, extra, *stats):
    shape = stats[0].shape
    groups = len(quarters)
    types = [f32] * 4 + [bf16]
    steps = len(spans_of(shape[0]))
    return pl.pallas_call(
        functools.partial(update_kernel, shape[0], groups),
        in_specs=[SMEM] + [VMEM_BLOCK] * (groups + 1) + [HBM] * 5,
        out_specs=[HBM] * 5 + [VMEM_BLOCK] * 2,
        out_shape=[pltpu.HBM(shape, kind) for kind in types]
        + [
            pltpu.VMEM((extra, HALF, 128), f32),
            pltpu.VMEM((1, 128), f32),
        ],
        scratch_shapes=[pltpu.VMEM(shape, f32)] * 5
        + [pltpu.VMEM(shape, kind) for kind in types]
        + [
            pltpu.SemaphoreType.DMA((5 * steps,)),
            pltpu.SemaphoreType.DMA((5 * steps,)),
        ],
        compiler_params=roomy(20),
        name="update",
    )(spot, *held_in(pltpu.VMEM, norm, *quarters), *held_in(pltpu.HBM, *stats))


def share_out(pieces, axis):
    return lax.all_to_all(pieces, axis, split_axis=0, concat_axis=0, tiled=True)


def swap(piece, distance):
    count = lax.axis_size("tile")
    return lax.ppermute(piece, "tile", [(i, i ^ distance) for i in range(count)])


def on_device(
    pixels,
    buckets,
    slot_owner_table,
    out_grad,
    master,
    left_stat,
    right_stat,
    left_root,
    right_root,
    vectors,
    moment,
):
    tile_count = lax.axis_size("tile")
    tile_place = lax.axis_index("tile")
    slot_count = pixels.shape[2]
    group_count = tile_count // STRIPS
    pairs = group_count // 2
    owned = master.shape[0]
    slots = owned * tile_count
    batch_count = lax.axis_size("batch")
    spot = lax.axis_index("batch").astype(jnp.int32).reshape(1)
    extra = extra_of(owned, batch_count)
    place = tile_place.astype(jnp.int32).reshape(1)
    paired = tile_count == 8
    numbers = jnp.arange(slots, dtype=jnp.int32)
    slot_of = jnp.sum(
        jnp.where(slot_owner_table[None, :] == numbers[:, None], numbers[None, :], 0), axis=1
    )
    if paired:
        owner = slot_of // owned
        apart = owner ^ tile_place
        apart = (apart & 1) * (tile_count // 2) + (apart >> 1)
        slot_of = slot_of + owned * (apart - owner)
    half = slots // 2
    near_place = jnp.where(slot_of < half, slot_of, half)
    far_place = jnp.where(slot_of < half, half, slot_of - half)
    vec = vectors.reshape(-1, 128)
    turned = lax.dynamic_index_in_dim(
        buckets.reshape(group_count, slot_count), tile_place, 1, keepdims=False
    ) >= 2
    flips = turned.reshape(-1, 1, 1, 1)
    goal = out_grad.reshape(2 * pairs, H3, W3, C3)
    goal = jnp.where(flips, goal.transpose(0, 2, 1, 3), goal)[:, :LINES]
    goal = goal.reshape(pairs, 2, LINES, W3, C3).transpose(0, 2, 3, 1, 4)
    goal = goal.reshape(pairs, LINES, 2 * W3, C3)
    goal = jnp.pad(goal, ((0, 0), (0, 0), (0, LINE - 2 * W3), (0, WIDE - C3)))
    goal = goal.reshape(pairs, AREA, WIDE)

    if paired:
        own, for_x, for_y, for_both = pack_pieces(
            place, master, pixels[0, 0].transpose(1, 2, 0, 3)
        )
        goal, vec, slot_of, near_place, far_place, for_both = lax.optimization_barrier(
            (goal, vec, slot_of, near_place, far_place, for_both)
        )
        from_x, from_y, strips_both = swap(for_x, 2), swap(for_y, 4), swap(for_both, 6)
        near_half = (owned + 1) // 2
        middle = STRIP_ROWS + near_half * HALF
        first_half = swap(from_x[STRIP_ROWS:middle], 4)
        second_half = swap(from_y[middle : STRIP_ROWS + owned * HALF], 2)
        mine = [own, from_x, from_y, strips_both, first_half, second_half]
        both = mine + [swap(piece, 1) for piece in mine]
        strips = both[:4] + both[6:10]
        pieces = [both[n] for n in (0, 1, 2, 4, 5, 6, 7, 8, 10, 11)]
        spans = [(STRIP_ROWS, owned)] * 3 + [(0, near_half), (0, owned - near_half)]
        spans = spans * 2
    else:
        pieces = [lax.all_gather(pack(master), "tile", axis=0, tiled=True).reshape(-1, 2 * BS)]
        spans = [(0, slots)]
        strips = share_out(pixels.reshape(tile_count, STRIP, C2), "tile")
        strips = [jnp.pad(strips, ((0, 0), (0, STRIP_ROWS - STRIP), (0, 0)))]

    weights = run_unpack(slot_of, pieces, spans)
    state = run_entry(place, buckets, strips, vec, tile_count)
    result, *back, near, far, flat = run_main(
        (near_place, far_place),
        place,
        buckets,
        state,
        goal,
        vec,
        weights,
        tile_count,
    )
    pixel_back, vector = run_exit(place, buckets, state, back, flat, vec, tile_count)
    if paired:
        own, *parts = fold_pair(near, swap(far, 1), tile_count // 2)
        pieces = [own] + [swap(part, 2 * k + 2) for k, part in enumerate(parts)]
        vector, _ = lax.optimization_barrier((vector, parts[0]))
        vector = vector + swap(vector, 1)
        vectors_in = [vector] + [swap(vector, 2 * k) for k in range(1, tile_count // 2)]
    else:
        outgoing = jnp.concatenate([near[:half], far[:half]], axis=0)
        pieces = list(share_out(outgoing.reshape(tile_count, owned, HALF, 128), "tile"))
        vectors_in = list(lax.all_gather(vector, "tile"))
    result, pieces[1] = lax.optimization_barrier((result, pieces[1]))
    result = result.reshape(pairs, LINES, LINE, WIDE)[:, :, : 2 * W3, :C3]
    result = result.reshape(pairs, LINES, W3, 2, C3).transpose(0, 3, 1, 2, 4)
    result = result.reshape(2 * pairs, LINES, W3, C3)
    result = jnp.pad(result, ((0, 0), (0, H3 - LINES), (0, 0), (0, 0)))
    result = jnp.where(flips, result.transpose(0, 2, 1, 3), result)
    result = result.reshape(out_grad.shape)
    result = with_layout_constraint(result, Layout(major_to_minor=(0, 1, 2, 4, 5, 3, 6)))
    result, vectors_in[0] = lax.optimization_barrier((result, vectors_in[0]))
    own, *parts = fold_tile(spot, pieces, vectors_in, extra, batch_count)
    pixel_back, parts[0] = lax.optimization_barrier((pixel_back, parts[0]))
    returned = share_out(pixel_back, "tile")
    parts = [
        lax.ppermute(part, "batch", [(i, (i + k + 1) % batch_count) for i in range(batch_count)])
        for k, part in enumerate(parts)
    ]
    quarter, norm = fold_batch(spot, [own] + parts, owned, tile_count)
    returned, norm = lax.optimization_barrier((returned, norm))
    norm = share_out(norm, ("batch", "tile"))
    returned = returned.astype(f32).reshape(pixels.shape)
    returned = with_layout_constraint(returned, Layout(major_to_minor=(0, 1, 3, 4, 2, 5)))
    returned, norm = lax.optimization_barrier((returned, norm))
    quarters = [quarter] + [
        lax.ppermute(quarter, "batch", [(i, (i + k) % batch_count) for i in range(batch_count)])
        for k in range(1, batch_count)
    ]
    block_grad, left_new, right_new, master_new, weight_copy, whole_vector, clip = update(
        spot, norm, quarters, extra, master, left_stat, right_stat, left_root, right_root
    )
    clip_norm = clip[0, 0]
    share = vectors.shape[0] // tile_count
    whole_vector = whole_vector.reshape(-1)
    vec_grad = lax.dynamic_slice_in_dim(whole_vector, tile_place * share, share, 0)
    vec_moment = moment + vec_grad * vec_grad
    own_vectors = lax.dynamic_slice_in_dim(vectors, tile_place * share, share, 0)
    vec_new = own_vectors - rate_vector * vec_grad / (jnp.sqrt(vec_moment) + eps_adagrad)
    return (
        result,
        returned,
        clip_norm,
        block_grad,
        left_new,
        right_new,
        master_new,
        weight_copy,
        vec_grad,
        vec_moment,
        vec_new,
    )


def solution(mesh):
    placed = (
        P("batch", "tile", None, None, None, None),
        P("batch"),
        P(),
        P("batch", "tile", None, None, None, None, None),
        P("tile", None, None),
        P("tile", None, None),
        P("tile", None, None),
        P("tile", None, None),
        P("tile", None, None),
        P(),
        P("tile"),
    )
    return jax.shard_map(
        on_device,
        mesh=mesh,
        in_specs=placed,
        out_specs=(
            P("batch", "tile", None, None, None, None, None),
            P("batch", "tile", None, None, None, None),
            P(),
            P("tile", None, None),
            P("tile", None, None),
            P("tile", None, None),
            P("tile", None, None),
            P("tile", None, None),
            P("tile"),
            P("tile"),
            P("tile"),
        ),
        check_vma=False,
    )
```

```python
import functools

import jax
import jax.numpy as jnp
from jax import lax
from jax.experimental import pallas as pl
from jax.experimental.layout import Layout, with_layout_constraint
from jax.experimental.pallas import tpu as pltpu
from jax.sharding import PartitionSpec as P

C2 = 128
HID2 = 512
C3 = 320
HID3 = 1280
CH = 36
CW = 36
STRIPS = 4
BS = 64
SR = CH // STRIPS
H3 = CH // 2
W3 = CW // 2
LONG = 7 * CH // 9
LINES = LONG // 2
WIDE = 384
LINE = 40
AREA = LINES * LINE
STEP = 2 * LINE
STEPS = AREA // STEP
HALF = BS // 2
STRIP = SR * CW
STRIP_ROWS = STRIP + -STRIP % 16

eps_norm = 1e-05
clip_limit = 1.0
rate_matrix = 0.3
rate_vector = 0.3
eps_adagrad = 1e-08
f32 = jnp.float32
bf16 = jnp.bfloat16

SHAPES = [(C2, HID2), (HID2, C2), (9 * C2, C3), (C3, HID3), (HID3, C3)]
USED = sum(rows // BS * (cols // BS) for rows, cols in SHAPES)
VEC_ROWS = (6 * C2 + HID2 + C2 + C3 + 6 * C3 + HID3 + C3) // 128


VEC_BLOCKS = -(-VEC_ROWS // HALF)


def extra_of(owned, groups):
    return VEC_BLOCKS + -(owned + VEC_BLOCKS) % groups


def product(left, right):
    return jnp.dot(left, right, preferred_element_type=f32)


def product_nt(left, right):
    return lax.dot_general(left, right, (((1,), (1,)), ((), ())), preferred_element_type=f32)


def product_tn(left, right):
    return lax.dot_general(left, right, (((0,), (0,)), ((), ())), preferred_element_type=f32)


def gelu_pair(values):
    bell = jnp.exp2(values * values * (-0.5 * 1.4426950408889634))
    step = pl.reciprocal(1.0 + (0.3275911 * 0.7071067811865476) * jnp.abs(values), approx=True)
    tail = step * (
        0.5 * 0.254829592
        + step
        * (
            0.5 * -0.284496736
            + step
            * (0.5 * 1.421413741 + step * (0.5 * -1.453152027 + step * (0.5 * 1.061405429)))
        )
    )
    tail = tail * bell
    share = jnp.where(values >= 0.0, 1.0 - tail, tail)
    return (values * share, share + values * (bell * 0.3989422804014327))


def fold(values):
    chans = values.shape[-1]
    return jnp.sum(values.reshape(-1, 8, chans), axis=0)


def by_image(total):
    total = total + pltpu.roll(total, 4, 0)
    total = total + pltpu.roll(total, 2, 0)
    return jnp.sum(total, axis=1, keepdims=True)


def line(pattern):
    return jnp.concatenate([pattern] * (LINE // 8), axis=0)


def spread(pattern, chans):
    return jnp.broadcast_to(pattern, (8, chans))


def affine(values, factor, shift):
    tiles = values.reshape(-1, 8, values.shape[-1])
    return (tiles * factor + shift).reshape(values.shape)


def scaled(values, factor):
    tiles = values.reshape(-1, 8, values.shape[-1])
    return (tiles * factor).reshape(values.shape)


def from_left(values):
    return pltpu.roll(values, 2, 0)


def from_right(values):
    return pltpu.roll(values, values.shape[0] - 2, 0)


def rounded(values):
    return values.astype(bf16).astype(f32)


def widen(values):
    return jnp.concatenate([values] * (WIDE // 128), axis=-1)


def norm_terms(total, square, count):
    mean = by_image(total) / count
    scaling = lax.rsqrt(by_image(square) / count - mean * mean + eps_norm)
    return (mean, scaling)


def sweep(visit, start):
    return lax.fori_loop(0, STEPS, visit, start, unroll=True)


def step_rows(k, lines=0):
    start = k * STEP + lines * LINE
    return pl.ds(start if isinstance(k, int) else pl.multiple_of(start, LINE), STEP)


def held_in(space, *arrays):
    return [pltpu.with_memory_space_constraint(array, space) for array in arrays]


VMEM_BLOCK = pl.BlockSpec(memory_space=pltpu.VMEM)
HBM = pl.BlockSpec(memory_space=pltpu.HBM)
SMEM = pl.BlockSpec(memory_space=pltpu.SMEM)


def roomy(mebibytes):
    return pltpu.CompilerParams(vmem_limit_bytes=mebibytes * 1024 * 1024)


def image_shape(bucket_of, pair, image):
    bucket = bucket_of(2 * pair + image)
    plain = jnp.where(bucket == 0, 5 * CH // 9, 7 * CH // 9)
    across = jnp.where(bucket == 0, CW, 7 * CW // 9)
    turned = (bucket >= 2).astype(jnp.int32)
    return (
        jnp.where(turned > 0, 5 * CW // 9, plain),
        jnp.where(turned > 0, CH, across),
        turned,
    )


def bucket_reader(place_ref, bucket_ref, strip_count):
    return lambda group: bucket_ref[group * strip_count + place_ref[0]]


class Geometry:
    def __init__(self, bucket_of, pair):
        parity = lax.broadcasted_iota(jnp.int32, (8, 128), 0) % 2
        even, odd = (image_shape(bucket_of, pair, image) for image in range(2))
        high, broad, turned = (jnp.where(parity == 0, a, b) for a, b in zip(even, odd))
        self.high = high
        self.count_two = (high * broad * C2).astype(f32)[:, :1]
        self.high3 = (high + 1) // 2
        broad3 = (broad + 1) // 2
        self.count_three = (self.high3 * broad3 * C3).astype(f32)[:, :1]
        place = lax.broadcasted_iota(jnp.int32, (LINE, 128), 0) // 2
        inside = lax.broadcasted_iota(jnp.int32, (LINE, 128), 0) < 2 * W3
        self.reach = []
        self.col_share = []
        for pc in range(2):
            column = 2 * place + pc
            self.reach.append(jnp.where(inside & (column < line(broad)), line(high), 0))
            edge = (column == 0) | (column == line(broad) - 1)
            self.col_share.append(jnp.where(edge, 0.5, 1.0 / 3.0))
        self.reach3 = jnp.where(inside & (place < line(broad3)), line(self.high3), 0)
        edge3 = (place == 0) | (place == line(broad3) - 1)
        self.col_share3 = jnp.where(edge3, 0.5, 1.0 / 3.0)
        self.flipped = jnp.concatenate([turned] * (STEP // 8), axis=0) > 0

    def share(self, plane, k):
        pr, pc = plane // 2, plane % 2
        return self.lines(4 * k + pr, 2, self.reach[pc], self.col_share[pc], self.high)

    def share3(self, k):
        return self.lines(2 * k, 1, self.reach3, self.col_share3, self.high3)

    def lines(self, row, stride, reach, col_share, height):
        parts = []
        for n in range(2):
            here = row + stride * n
            row_share = jnp.where((here == 0) | (here == height - 1), 0.5, 1.0 / 3.0)
            parts.append(jnp.where(here < reach, line(row_share) * col_share, 0.0))
        return jnp.concatenate(parts, axis=0)


def strip_place(pair, spot, strip_count):
    return lax.rem(pair * 8 + strip_count - 2 + spot, strip_count)


def each_image(bucket_of, pair, visit):
    for image in range(2):
        way = image_shape(bucket_of, pair, image)[2]

        @pl.when(way == 0)
        def _():
            def one(r, carry):
                for plane in range(4):
                    row = 2 * r + plane // 2
                    strip = row // SR
                    there = pl.ds((row - strip * SR) * CW + plane % 2, W3, stride=2)
                    here = pl.ds(r * LINE + image, W3, stride=2)
                    visit(plane, here, image * STRIPS + strip, there)
                return carry

            lax.fori_loop(0, LINES, one, 0)

        @pl.when(way == 1)
        def _():
            def one(r, carry):
                for plane in range(4):
                    for strip in range(STRIPS):
                        first = (plane % 2 + strip * SR) % 2
                        count = (SR - first + 1) // 2
                        done = (strip * SR + first) // 2
                        column = 2 * r + plane // 2
                        there = pl.ds(first * CW + column, count, stride=2 * CW)
                        here = pl.ds(r * LINE + image + 2 * done, count, stride=2)
                        visit(plane, here, image * STRIPS + strip, there)
                return carry

            lax.fori_loop(0, LINES, one, 0)


def row_windows(col_ref, pc, k):
    both = col_ref[pc, step_rows(k, 1)] + col_ref[2 + pc, step_rows(k, 1)]
    return (both + col_ref[2 + pc, step_rows(k)], both + col_ref[pc, step_rows(k, 2)])


def put_col_windows(col_ref, pr, k, even, odd):
    both = even + odd
    col_ref[pr * 2, step_rows(k, 1)] = both + from_left(odd)
    col_ref[pr * 2 + 1, step_rows(k, 1)] = both + from_right(even)


def clear_edges(col_ref):
    zero_line = jnp.zeros((LINE, C2), f32)
    for plane in range(4):
        col_ref[plane, 0:LINE] = zero_line
        col_ref[plane, AREA + LINE : AREA + 2 * LINE] = zero_line


def entry_kernel(pairs, strip_count, piece_count, place_ref, bucket_ref, vec_ref, *refs):
    piece_refs, refs = refs[:piece_count], refs[piece_count:]
    x_out, inv_out, pool_out, mix_out, stat_out, image_ref, col_ref = refs
    pair = pl.program_id(0) if pairs > 1 else 0
    x_ref, inv_ref, pool_ref, mix_ref = (ref.at[0] for ref in (x_out, inv_out, pool_out, mix_out))
    bucket_of = bucket_reader(place_ref, bucket_ref, strip_count)
    shape = Geometry(bucket_of, pair)
    gain1, bias1, scale1 = (vec_ref[n : n + 1] for n in range(3))
    clear_edges(col_ref)
    if piece_count > 1:
        half = piece_count // 2
        for n, ref in enumerate(piece_refs):
            source = place_ref[0] ^ (n // half + 2 * (n % half))
            spot = lax.rem(source + 2, 2 * STRIPS)
            first = 0 if n < half else ref.shape[0] - STRIP_ROWS
            image_ref[spot] = ref[first : first + STRIP_ROWS].astype(f32)
    else:
        for spot in range(2 * STRIPS):
            source = strip_place(pair, spot, strip_count)
            image_ref[spot] = piece_refs[0][source].astype(f32)

    def take_in(plane, here, spot, there):
        x_ref[plane, here] = image_ref[spot, there]

    each_image(bucket_of, pair, take_in)

    def arrange(k, carry):
        total, square = carry
        rows = step_rows(k)
        for plane in range(4):
            share = shape.share(plane, k)
            inv_ref[plane, rows] = share
            values = jnp.where(share > 0.0, x_ref[plane, rows], 0.0)
            x_ref[plane, rows] = values
            total = total + fold(values)
            square = square + fold(values * values)
        return (total, square)

    nothing = jnp.zeros((8, C2), f32)
    total, square = sweep(arrange, (nothing, nothing))
    mean1, scaling1 = norm_terms(total, square, shape.count_two)
    factor1 = scaling1 * gain1
    shift1 = bias1 - mean1 * scaling1 * gain1

    def window_cols(k, carry):
        rows = step_rows(k)
        for pr in range(2):
            masked = []
            for pc in range(2):
                plane = pr * 2 + pc
                normal = rounded(affine(x_ref[plane, rows], factor1, shift1))
                masked.append(jnp.where(inv_ref[plane, rows] > 0.0, normal, 0.0))
            put_col_windows(col_ref, pr, k, *masked)
        return carry

    sweep(window_cols, 0)

    def mix(k, carry):
        total, square = carry
        rows = step_rows(k)
        for pc in range(2):
            windows = row_windows(col_ref, pc, k)
            for pr in range(2):
                plane = pr * 2 + pc
                values = x_ref[plane, rows]
                share = inv_ref[plane, rows]
                pooled = windows[pr] * share - rounded(affine(values, factor1, shift1))
                pooled = jnp.where(share > 0.0, pooled, 0.0)
                mixed = values + scale1 * pooled
                pool_ref[plane, rows] = pooled
                mix_ref[plane, rows] = mixed
                total = total + fold(mixed)
                square = square + fold(mixed * mixed)
        return (total, square)

    total, square = sweep(mix, (nothing, nothing))
    mean2, scaling2 = norm_terms(total, square, shape.count_two)
    for n, value in enumerate((mean1, scaling1, mean2, scaling2)):
        stat_out[0, n] = spread(value, 128)


def pair_specs(pairs, shapes, mode=None):
    if pairs == 1:
        return [VMEM_BLOCK] * len(shapes)
    return [
        pl.BlockSpec(
            (1,) + shape, lambda t, rank=len(shape): (t,) + (0,) * rank, pipeline_mode=mode
        )
        for shape in shapes
    ]


def whole_specs(pairs, shapes):
    if pairs == 1:
        return [VMEM_BLOCK] * len(shapes)
    return [
        pl.BlockSpec(
            shape,
            lambda t, rank=len(shape): (0,) * rank,
            pipeline_mode=pl.Buffered(1),
        )
        for shape in shapes
    ]


def pair_arrays(pairs, shapes, kinds):
    make = pltpu.VMEM if pairs == 1 else jax.ShapeDtypeStruct
    return [make((pairs,) + shape, kind) for shape, kind in zip(shapes, kinds)]


STATE = [(4, AREA, C2)] * 4 + [(4, 8, 128)]
BACK = [(4, AREA, C2)] * 2 + [(2, 8, 128)]


def run_entry(place, buckets, pieces, vec, strip_count):
    pairs = strip_count // 8
    if pairs == 1:
        pieces = held_in(pltpu.VMEM, *pieces)
    return pl.pallas_call(
        functools.partial(entry_kernel, pairs, strip_count, len(pieces)),
        grid=() if pairs == 1 else (pairs,),
        in_specs=[SMEM] * 2 + whole_specs(pairs, [array.shape for array in (vec, *pieces)]),
        out_specs=pair_specs(pairs, STATE),
        out_shape=pair_arrays(pairs, STATE, [f32] * 5),
        scratch_shapes=[
            pltpu.VMEM((2 * STRIPS, STRIP_ROWS, C2), f32),
            pltpu.VMEM((4, AREA + 2 * LINE, C2), f32),
        ],
        compiler_params=roomy(6 if pairs == 1 else 40),
        name="entry",
    )(place, buckets, vec, *pieces)


WEIGHTS = [(C2, HID2), (HID2, C2), (9 * C2, WIDE), (WIDE, HID3), (HID3, WIDE)]


def unpack_kernel(spans, slot_ref, *refs):
    piece_refs, refs = refs[: len(spans)], refs[len(spans) :]
    weights, gathered_ref = refs[:-1], refs[-1]
    done = 0
    for ref, (first, count) in zip(piece_refs, spans):
        blocks = ref[first : first + count * HALF].reshape(count, HALF, 128)
        gathered_ref[done : done + count] = blocks
        done += count
    left_half = lax.broadcasted_iota(jnp.int32, (HALF, 128), 1) < BS
    offset = 0
    for (rows, cols), ref in zip(SHAPES, weights):
        wide = cols // BS
        for rb in range(rows // BS):
            for cb in range(0, wide, 2):
                number = offset + rb * wide + cb
                first = gathered_ref[slot_ref[number]]
                turned = pltpu.roll(first, BS, 1)
                if cb + 1 < wide:
                    second = gathered_ref[slot_ref[number + 1]]
                    top = jnp.where(left_half, first, pltpu.roll(second, BS, 1))
                    low = jnp.where(left_half, turned, second)
                else:
                    top = jnp.where(left_half, first, 0.0)
                    low = jnp.where(left_half, turned, 0.0)
                place = slice(cb * BS, cb * BS + 128)
                ref[rb * BS : rb * BS + HALF, place] = top
                ref[rb * BS + HALF : rb * BS + BS, place] = low
        offset += rows // BS * wide
    weights[3][C3:, :] = jnp.zeros((WIDE - C3, HID3), bf16)


def run_unpack(slot_of, pieces, spans):
    slots = slot_of.shape[0]
    return pl.pallas_call(
        functools.partial(unpack_kernel, spans),
        in_specs=[SMEM] + [VMEM_BLOCK] * len(pieces),
        out_specs=[VMEM_BLOCK] * 5,
        out_shape=[pltpu.VMEM(shape, bf16) for shape in WEIGHTS],
        scratch_shapes=[pltpu.VMEM((slots, HALF, 128), bf16)],
        compiler_params=roomy(6),
        name="unpack",
    )(slot_of, *held_in(pltpu.VMEM, *pieces))


def main_kernel(
    pairs,
    strip_count,
    slots,
    near_place,
    far_place,
    place_ref,
    bucket_ref,
    inv_in,
    mix_in,
    stat_in,
    goal_ref,
    vec_ref,
    w1_ref,
    w2_ref,
    we_ref,
    w3_ref,
    w4_ref,
    result_ref,
    zed_out,
    dx_out,
    mean_out,
    near_ref,
    far_ref,
    flat_ref,
    zed_ref,
    hid_ref,
    u_ref,
    g_ref,
    h_ref,
    dy_ref,
    patch_ref,
    dpatch_ref,
    inv3_ref,
    e_ref,
    col3_ref,
    pool3_ref,
    mix3_ref,
    dx3_ref,
    hid3_ref,
    dhid3_ref,
    u3_ref,
    g3_ref,
    h3_ref,
    dy3_ref,
    dpre_ref,
    gw1_ref,
    gw2_ref,
    gwe_ref,
    gw3_ref,
    gw4_ref,
    acc_two,
    acc_hid_two,
    acc_three,
    acc_hid_three,
):
    pair = pl.program_id(0) if pairs > 1 else 0
    grads = [gw1_ref, gw2_ref, gwe_ref, gw3_ref, gw4_ref]
    inv_ref, mix_ref, stat_ref = (ref.at[0] for ref in (inv_in, mix_in, stat_in))
    back_ref, dx_ref = zed_out.at[0], dx_out.at[0]
    left_half = lax.broadcasted_iota(jnp.int32, (HALF, 128), 1) < BS

    def at_pair(number, act):
        if pairs == 1:
            act()
        else:
            pl.when(pair == number)(act)

    def begin():
        acc_two[...] = jnp.zeros(acc_two.shape, f32)
        acc_hid_two[...] = jnp.zeros(acc_hid_two.shape, f32)
        acc_three[...] = jnp.zeros(acc_three.shape, f32)
        acc_hid_three[...] = jnp.zeros(acc_hid_three.shape, f32)

    at_pair(0, begin)
    shape = Geometry(bucket_reader(place_ref, bucket_ref, strip_count), pair)
    count_two, count_three, flipped = shape.count_two, shape.count_three, shape.flipped
    nothing = jnp.zeros((8, C2), f32)
    nothing3 = jnp.zeros((8, WIDE), f32)

    def vector_row(at, length):
        first, shift = at // 128, at % 128
        count = -(-(shift + length) // 128)
        row = jnp.concatenate([vec_ref[first + n : first + n + 1] for n in range(count)], axis=1)
        if shift:
            row = pltpu.roll(jnp.broadcast_to(row, (8, count * 128)), count * 128 - shift, 1)[:1]
        return row

    def wide_row(at):
        lane = lax.broadcasted_iota(jnp.int32, (1, WIDE), 1)
        return jnp.where(lane < C3, vector_row(at, C3)[:, :WIDE], 0.0)

    gain2, bias2, scale2 = (vec_ref[n : n + 1] for n in range(3, 6))
    hid_bias = vector_row(6 * C2, HID2)
    out_bias = vector_row(6 * C2 + HID2, C2)
    two = 7 * C2 + HID2
    embed_bias, gain3, bias3, scale3 = (wide_row(two + n * C3) for n in range(4))
    gain4, bias4, scale4 = (wide_row(two + n * C3) for n in range(4, 7))
    hid_bias3 = vector_row(two + 7 * C3, HID3)[:, :HID3]
    out_bias3 = wide_row(two + 7 * C3 + HID3)
    mean2, scaling2 = stat_ref[2], stat_ref[3]
    factor2 = scaling2 * gain2
    shift2 = bias2 - mean2 * scaling2 * gain2
    for plane in range(4):
        zed_ref[plane, 0:LINE] = jnp.zeros((LINE, C2), f32)
    col3_ref[0:LINE] = jnp.zeros((LINE, WIDE), f32)
    col3_ref[AREA + LINE : AREA + 2 * LINE] = jnp.zeros((LINE, WIDE), f32)

    def put_block(number, block):
        near_ref[near_place[number]] = block
        far_ref[far_place[number]] = block

    offsets = [0]
    for rows, cols in SHAPES:
        offsets.append(offsets[-1] + rows // BS * (cols // BS))

    def pack_part(which, values, row=0, col=0):
        rows, cols = SHAPES[which]
        wide = cols // BS
        values = values.astype(bf16)
        for rb in range(row // BS, min(rows, row + values.shape[0]) // BS):
            for cb in range(col // BS, min(cols, col + values.shape[1]) // BS, 2):
                number = offsets[which] + rb * wide + cb
                start = rb * BS - row
                at = slice(cb * BS - col, cb * BS - col + 128)
                top = values[start : start + HALF, at]
                low = values[start + HALF : start + BS, at]
                put_block(number, jnp.where(left_half, top, pltpu.roll(low, BS, 1)))
                if cb + 1 < wide:
                    put_block(number + 1, jnp.where(left_half, pltpu.roll(top, BS, 1), low))

    def plane_rows(plane):
        return slice(plane * AREA, plane * AREA + AREA)

    def begin_plane(plane):
        low = affine(mix_ref[plane], factor2, shift2).astype(bf16)
        h_ref[plane_rows(plane)] = low
        hid_ref[plane % 2] = product(low, w1_ref[...])

    begin_plane(0)
    for plane in range(4):
        if plane < 3:
            begin_plane(plane + 1)
        for k in range(STEPS):
            rows = step_rows(k)
            flat = slice(plane * AREA + k * STEP, plane * AREA + k * STEP + STEP)
            for at in range(0, HID2, 128):
                lanes = slice(at, at + 128)
                active, slope = gelu_pair(hid_ref[plane % 2, rows, lanes] + hid_bias[:, lanes])
                u_ref[flat, lanes] = active.astype(bf16)
                g_ref[flat, lanes] = slope.astype(bf16)
        out = product(u_ref[plane_rows(plane)], w2_ref[...]) + out_bias
        zed = jnp.where(inv_ref[plane] > 0.0, mix_ref[plane] + scale2 * out, 0.0)
        zed_ref[plane, LINE : LINE + AREA] = rounded(zed)

    def patches(k, carry):
        rows = step_rows(k)
        taps = []
        for ky in range(3):
            pr = (0 if ky == 1 else 1) * 2
            source = step_rows(k, 0 if ky == 0 else 1)
            even = zed_ref[pr, source]
            odd = zed_ref[pr + 1, source]
            taps.append((from_left(odd), even, odd))
        for ky in range(3):
            for kx in range(3):
                at = (3 * ky + kx) * C2
                tap = taps[ky][kx]
                if ky != kx:
                    tap = jnp.where(flipped, taps[kx][ky], tap)
                patch_ref[rows, at : at + C2] = tap.astype(bf16)
        return carry

    sweep(patches, 0)
    e_ref[...] = product(patch_ref[...], we_ref[...])

    def embed(k, carry):
        total, square = carry
        rows = step_rows(k)
        share = shape.share3(k)
        inv3_ref[rows] = share
        out = jnp.where(widen(share) > 0.0, e_ref[rows] + embed_bias, 0.0)
        e_ref[rows] = out
        return (total + fold(out), square + fold(out * out))

    total, square = sweep(embed, (nothing3, nothing3))
    mean3, scaling3 = norm_terms(total, square, count_three)
    factor3 = scaling3 * gain3
    shift3 = bias3 - mean3 * scaling3 * gain3

    def window_cols3(k, carry):
        rows = step_rows(k)
        normal = rounded(affine(e_ref[rows], factor3, shift3))
        masked = jnp.where(widen(inv3_ref[rows]) > 0.0, normal, 0.0)
        col3_ref[step_rows(k, 1)] = masked + from_left(masked) + from_right(masked)
        return carry

    sweep(window_cols3, 0)

    def row_windows3(k):
        return col3_ref[step_rows(k)] + col3_ref[step_rows(k, 1)] + col3_ref[step_rows(k, 2)]

    def mix3(k, carry):
        total, square = carry
        rows = step_rows(k)
        values = e_ref[rows]
        share = widen(inv3_ref[rows])
        pooled = row_windows3(k) * share - rounded(affine(values, factor3, shift3))
        pooled = jnp.where(share > 0.0, pooled, 0.0)
        mixed = values + scale3 * pooled
        pool3_ref[rows] = pooled
        mix3_ref[rows] = mixed
        return (total + fold(mixed), square + fold(mixed * mixed))

    total, square = sweep(mix3, (nothing3, nothing3))
    mean4, scaling4 = norm_terms(total, square, count_three)
    factor4 = scaling4 * gain4
    shift4 = bias4 - mean4 * scaling4 * gain4
    normal4 = (spread(scaling4, WIDE), spread(-mean4 * scaling4, WIDE))

    def prepare3(k, d_bias):
        rows = step_rows(k)
        h3_ref[rows] = affine(mix3_ref[rows], factor4, shift4).astype(bf16)
        goal = goal_ref[0, rows].astype(f32)
        goal = jnp.where(widen(inv3_ref[rows]) > 0.0, goal, 0.0)
        goal = scale4 * goal
        dy3_ref[rows] = goal.astype(bf16)
        return d_bias + fold(goal)

    acc_three[7] += sweep(prepare3, nothing3)

    def keep(which, value, row=0, col=0):
        if pairs == 1:
            pack_part(which, value, row, col)
        else:
            ref = grads[which]
            place = (slice(row, row + value.shape[0]), slice(col, col + value.shape[1]))

            @pl.when(pair == 0)
            def _():
                ref[place] = value

            @pl.when(pair > 0)
            def _():
                ref[place] += value

    def begin_chunk(at):
        lanes = slice(at, at + 256)
        hid3_ref[:, lanes] = product(h3_ref[...], w3_ref[:, lanes])
        dhid3_ref[:, lanes] = product_nt(dy3_ref[...], w4_ref[lanes])

    begin_chunk(0)
    for at in range(0, HID3, 256):
        if at + 256 < HID3:
            begin_chunk(at + 256)
        for lane in (at, at + 128):
            lanes = slice(lane, lane + 128)
            total = nothing
            for k in range(STEPS):
                rows = step_rows(k)
                active, slope = gelu_pair(hid3_ref[rows, lanes] + hid_bias3[:, lanes])
                u3_ref[rows, lanes] = active.astype(bf16)
                change = slope * dhid3_ref[rows, lanes]
                g3_ref[rows, lanes] = change.astype(bf16)
                total = total + fold(change)
            acc_hid_three[:, lanes] += total
        lanes = slice(at, at + 256)
        out = product(u3_ref[:, lanes], w4_ref[lanes])
        d_low = product_nt(g3_ref[:, lanes], w3_ref[:, lanes])
        result_ref[0] = out if at == 0 else result_ref[0] + out
        dx3_ref[...] = d_low if at == 0 else dx3_ref[...] + d_low
        keep(3, product_tn(h3_ref[...], g3_ref[:, lanes]), col=at)
        keep(4, product_tn(u3_ref[:, lanes], dy3_ref[...]), row=at)

    def finish3(k, carry):
        d_scale, d_shift, d_gain = carry
        rows = step_rows(k)
        valid = widen(inv3_ref[rows]) > 0.0
        mixed = mix3_ref[rows]
        out = jnp.where(valid, result_ref[0, rows] + out_bias3, 0.0)
        result_ref[0, rows] = mixed + scale4 * out
        d_scale = d_scale + fold(out * goal_ref[0, rows].astype(f32))
        d_low = dx3_ref[rows]
        normal = affine(mixed, *normal4)
        return (d_scale, d_shift + fold(d_low), d_gain + fold(d_low * normal))

    d_scale, d_shift, d_gain = sweep(finish3, (nothing3, nothing3, nothing3))
    acc_three[6] += d_scale
    acc_three[5] += d_shift
    acc_three[4] += d_gain
    mean_shift = by_image(d_shift * gain4) / count_three
    mean_gain = by_image(d_gain * gain4) / count_three
    back_gain4 = scaling4 * gain4
    back_mean4 = spread(-scaling4 * mean_shift, WIDE)
    back_normal4 = spread(scaling4 * mean_gain, WIDE)

    def unmix3(k, d_scale):
        rows = step_rows(k)
        share = widen(inv3_ref[rows])
        valid = share > 0.0
        normal = affine(mix3_ref[rows], *normal4)
        back = affine(dx3_ref[rows], back_gain4, back_mean4) - scaled(normal, back_normal4)
        d_mixed = jnp.where(valid, back + goal_ref[0, rows].astype(f32), 0.0)
        dx3_ref[rows] = d_mixed
        d_scale = d_scale + fold(pool3_ref[rows] * d_mixed)
        weighted = scale3 * d_mixed * share
        col3_ref[step_rows(k, 1)] = weighted + from_left(weighted) + from_right(weighted)
        return d_scale

    acc_three[3] += sweep(unmix3, nothing3)
    normal3 = (spread(scaling3, WIDE), spread(-mean3 * scaling3, WIDE))

    def unpool3(k, carry):
        d_shift, d_gain = carry
        rows = step_rows(k)
        valid = widen(inv3_ref[rows]) > 0.0
        d_normal = jnp.where(valid, row_windows3(k) - scale3 * dx3_ref[rows], 0.0)
        pool3_ref[rows] = d_normal
        normal = affine(e_ref[rows], *normal3)
        return (d_shift + fold(d_normal), d_gain + fold(d_normal * normal))

    d_shift, d_gain = sweep(unpool3, (nothing3, nothing3))
    acc_three[2] += d_shift
    acc_three[1] += d_gain
    mean_shift = by_image(d_shift * gain3) / count_three
    mean_gain = by_image(d_gain * gain3) / count_three
    back_gain3 = scaling3 * gain3
    back_mean3 = spread(-scaling3 * mean_shift, WIDE)
    back_normal3 = spread(scaling3 * mean_gain, WIDE)

    def unnorm3(k, d_bias):
        rows = step_rows(k)
        valid = widen(inv3_ref[rows]) > 0.0
        normal = affine(e_ref[rows], *normal3)
        back = affine(pool3_ref[rows], back_gain3, back_mean3) - scaled(normal, back_normal3)
        low = jnp.where(valid, dx3_ref[rows] + back, 0.0).astype(bf16)
        dpre_ref[rows] = low
        return d_bias + fold(low.astype(f32))

    acc_three[0] += sweep(unnorm3, nothing3)
    keep(2, product_tn(patch_ref[...], dpre_ref[...]))
    dpatch_ref[0:AREA] = product_nt(dpre_ref[...], we_ref[...])
    dpatch_ref[AREA : AREA + LINE] = jnp.zeros((LINE, 9 * C2), f32)

    def gather_back(k, carry):
        rows = step_rows(k)

        def tap(ky, kx, source):
            at = (3 * ky + kx) * C2
            value = dpatch_ref[source, at : at + C2]
            if ky != kx:
                at = (3 * kx + ky) * C2
                value = jnp.where(flipped, dpatch_ref[source, at : at + C2], value)
            return value

        sources = []
        for ky in range(3):
            source = step_rows(k, 1 if ky == 0 else 0)
            sources.append(
                (tap(ky, 1, source), tap(ky, 2, source) + from_right(tap(ky, 0, source)))
            )
        for pc in range(2):
            for pr, value in ((0, sources[1][pc]), (1, sources[2][pc] + sources[0][pc])):
                plane = pr * 2 + pc
                valid = inv_ref[plane, rows] > 0.0
                back_ref[plane, rows] = jnp.where(valid, rounded(value), 0.0)
        return carry

    sweep(gather_back, 0)

    normal2 = (spread(scaling2, C2), spread(-mean2 * scaling2, C2))

    def begin_back(plane):
        goal = scale2 * back_ref[plane]
        dy_ref[plane_rows(plane)] = goal.astype(bf16)
        hid_ref[plane % 2] = product_nt(goal.astype(bf16), w2_ref[...])
        return fold(goal)

    d_out_bias = begin_back(0)
    d_shift, d_gain = nothing, nothing
    sums = [nothing] * (HID2 // 128)
    new_gw1, new_gw2 = None, None
    for plane in range(4):
        if plane < 3:
            d_out_bias = d_out_bias + begin_back(plane + 1)
        for k in range(STEPS):
            rows = step_rows(k)
            part = slice(plane * AREA + k * STEP, plane * AREA + k * STEP + STEP)
            for n, at in enumerate(range(0, HID2, 128)):
                lanes = slice(at, at + 128)
                change = g_ref[part, lanes].astype(f32) * hid_ref[plane % 2, rows, lanes]
                g_ref[part, lanes] = change.astype(bf16)
                sums[n] = sums[n] + fold(change)
        flat = plane_rows(plane)
        d_low = product_nt(g_ref[flat], w1_ref[...])
        dx_ref[plane] = d_low
        d_shift = d_shift + fold(d_low)
        d_gain = d_gain + fold(d_low * affine(mix_ref[plane], *normal2))
        part_gw1 = product_tn(h_ref[flat], g_ref[flat])
        part_gw2 = product_tn(dy_ref[flat], u_ref[flat])
        new_gw1 = part_gw1 if plane == 0 else new_gw1 + part_gw1
        new_gw2 = part_gw2 if plane == 0 else new_gw2 + part_gw2
    new_gw2 = new_gw2.T
    for n, value in enumerate(sums):
        acc_hid_two[:, n * 128 : n * 128 + 128] += value
    acc_two[6] += d_out_bias
    acc_two[4] += d_shift
    acc_two[3] += d_gain
    mean_out[0, 0] = spread(by_image(d_shift * gain2) / count_two, 128)
    mean_out[0, 1] = spread(by_image(d_gain * gain2) / count_two, 128)
    keep(0, new_gw1)
    keep(1, new_gw2)
    d_scale = fold(w2_ref[...].astype(f32) * new_gw2) + out_bias * d_out_bias
    acc_two[5] += d_scale / scale2

    def finish():
        if pairs > 1:
            for which, ref in enumerate(grads):
                pack_part(which, ref[...])

        def filler(number, carry):
            put_block(number, jnp.zeros((HALF, 128), bf16))
            return carry

        lax.fori_loop(USED, slots, filler, 0)

        flat_ref[...] = jnp.zeros(flat_ref.shape, f32)

        def put(at, total, length):
            if at % 128:
                room = jnp.zeros((8, 128), f32)
                if total.shape[1] < length + BS:
                    total = jnp.concatenate([total, room], axis=1)
                total = pltpu.roll(total, BS, 1)
            whole = jnp.sum(total, axis=0, keepdims=True)
            done = -(at % 128)
            row = at // 128
            lane = 0
            while done < length:
                first = max(0, -done)
                last = min(128, length - done)
                flat_ref[row : row + 1, first:last] = whole[:, lane + first : lane + last]
                done += 128
                lane += 128
                row += 1

        at = 3 * C2
        for n in range(3, 6):
            put(at, acc_two[n], C2)
            at += C2
        put(at, acc_hid_two[...], HID2)
        at += HID2
        put(at, acc_two[6], C2)
        at += C2
        for n in range(7):
            put(at, acc_three[n], C3)
            at += C3
        put(at, acc_hid_three[...], HID3)
        at += HID3
        put(at, acc_three[7], C3)

    at_pair(pairs - 1, finish)


def run_main(places, place, buckets, state, goal, vec, weights, strip_count):
    pairs = goal.shape[0]
    slots = places[0].shape[0]
    half = slots // 2 + 1
    if pairs == 1:
        state = held_in(pltpu.VMEM, *state)
    weights = held_in(pltpu.VMEM, *weights)
    _, inv, _, mix, stat = state
    state_shapes = [STATE[1], STATE[3], STATE[4]]
    wide_f32 = pltpu.VMEM((AREA, WIDE), f32)
    wide_bf16 = pltpu.VMEM((AREA, WIDE), bf16)
    scratch = [
        pltpu.VMEM((4, AREA + LINE, C2), f32),
        pltpu.VMEM((2, AREA, HID2), f32),
        pltpu.VMEM((4 * AREA, HID2), bf16),
        pltpu.VMEM((4 * AREA, HID2), bf16),
        pltpu.VMEM((4 * AREA, C2), bf16),
        pltpu.VMEM((4 * AREA, C2), bf16),
        pltpu.VMEM((AREA, 9 * C2), bf16),
        pltpu.VMEM((AREA + LINE, 9 * C2), f32),
        pltpu.VMEM((AREA, 128), f32),
        wide_f32,
        pltpu.VMEM((AREA + 2 * LINE, WIDE), f32),
        wide_f32,
        wide_f32,
        wide_f32,
        pltpu.VMEM((AREA, HID3), f32),
        pltpu.VMEM((AREA, HID3), f32),
        pltpu.VMEM((AREA, HID3), bf16),
        pltpu.VMEM((AREA, HID3), bf16),
        wide_bf16,
        wide_bf16,
        wide_bf16,
        *[pltpu.VMEM(shape if pairs > 1 else (8, 128), f32) for shape in WEIGHTS],
        pltpu.VMEM((7, 8, C2), f32),
        pltpu.VMEM((8, HID2), f32),
        pltpu.VMEM((8, 8, WIDE), f32),
        pltpu.VMEM((8, HID3), f32),
    ]
    out_shapes = [(half, HALF, 128), (half, HALF, 128), (VEC_BLOCKS * HALF, 128)]
    make = pltpu.VMEM if pairs == 1 else jax.ShapeDtypeStruct
    return pl.pallas_call(
        functools.partial(main_kernel, pairs, strip_count, slots),
        grid=() if pairs == 1 else (pairs,),
        in_specs=[SMEM] * 4
        + pair_specs(pairs, state_shapes + [goal.shape[1:]], pl.Buffered(1))
        + whole_specs(pairs, [vec.shape])
        + [VMEM_BLOCK] * 5,
        out_specs=pair_specs(pairs, [(AREA, WIDE)] + BACK) + whole_specs(pairs, out_shapes),
        out_shape=pair_arrays(pairs, [(AREA, WIDE)] + BACK, [f32] * 4)
        + [make(shape, kind) for shape, kind in zip(out_shapes, (bf16, bf16, f32))],
        scratch_shapes=scratch,
        compiler_params=pltpu.CompilerParams(
            vmem_limit_bytes=(40 if pairs == 1 else 56) * 1024 * 1024,
        ),
        name="blocks",
    )(*places, place, buckets, inv, mix, stat, goal, vec, *weights)


def exit_kernel(
    pairs,
    strip_count,
    place_ref,
    bucket_ref,
    x_in,
    inv_in,
    pool_in,
    mix_in,
    stat_in,
    zed_in,
    dx_in,
    mean_in,
    flat_ref,
    vec_ref,
    payload_hbm,
    vector_ref,
    payload_ref,
    image_ref,
    col_ref,
    dx_ref,
    back_ref,
    acc_ref,
    sem,
):
    pair = pl.program_id(0) if pairs > 1 else 0
    x_ref, inv_ref, pool_ref, mix_ref, stat_ref, zed_ref, low_ref, mean_ref = (
        ref.at[0] for ref in (x_in, inv_in, pool_in, mix_in, stat_in, zed_in, dx_in, mean_in)
    )
    bucket_of = bucket_reader(place_ref, bucket_ref, strip_count)
    shape = Geometry(bucket_of, pair)
    count_two = shape.count_two
    gain1, bias1, scale1, gain2 = (vec_ref[n : n + 1] for n in range(4))
    mean1, scaling1, mean2, scaling2 = (stat_ref[n] for n in range(4))
    normal2 = (scaling2, -mean2 * scaling2)
    clear_edges(col_ref)
    nothing = jnp.zeros((8, C2), f32)
    back_gain2 = scaling2 * gain2
    back_mean2 = -scaling2 * mean_ref[0]
    back_normal2 = scaling2 * mean_ref[1]

    if pairs > 1:

        @pl.when(pair == 0)
        def _():
            acc_ref[...] = jnp.zeros(acc_ref.shape, f32)

    def add_up(n, total):
        acc_ref[n] = total if pairs == 1 else acc_ref[n] + total

    def unmix(k, d_scale):
        rows = step_rows(k)
        for pr in range(2):
            weighted = []
            for pc in range(2):
                plane = pr * 2 + pc
                share = inv_ref[plane, rows]
                normal = affine(mix_ref[plane, rows], *normal2)
                back = affine(low_ref[plane, rows], back_gain2, back_mean2)
                back = back - scaled(normal, back_normal2)
                d_mixed = jnp.where(share > 0.0, zed_ref[plane, rows] + back, 0.0)
                dx_ref[plane, rows] = d_mixed
                d_scale = d_scale + fold(pool_ref[plane, rows] * d_mixed)
                weighted.append(scale1 * d_mixed * share)
            put_col_windows(col_ref, pr, k, *weighted)
        return d_scale

    add_up(2, sweep(unmix, nothing))
    normal1 = (spread(scaling1, C2), spread(-mean1 * scaling1, C2))

    def unpool(k, carry):
        d_shift, d_gain = carry
        rows = step_rows(k)
        for pc in range(2):
            windows = row_windows(col_ref, pc, k)
            for pr in range(2):
                plane = pr * 2 + pc
                valid = inv_ref[plane, rows] > 0.0
                d_normal = windows[pr] - scale1 * dx_ref[plane, rows]
                d_normal = jnp.where(valid, d_normal, 0.0)
                back_ref[plane, rows] = d_normal
                normal = affine(x_ref[plane, rows], *normal1)
                d_shift = d_shift + fold(d_normal)
                d_gain = d_gain + fold(d_normal * normal)
        return (d_shift, d_gain)

    d_shift, d_gain = sweep(unpool, (nothing, nothing))
    add_up(1, d_shift)
    add_up(0, d_gain)
    mean_shift = by_image(d_shift * gain1) / count_two
    mean_gain = by_image(d_gain * gain1) / count_two
    back_gain1 = scaling1 * gain1
    back_mean1 = spread(-scaling1 * mean_shift, C2)
    back_normal1 = spread(scaling1 * mean_gain, C2)

    def unnorm(k, carry):
        rows = step_rows(k)
        for plane in range(4):
            normal = affine(x_ref[plane, rows], *normal1)
            back = affine(back_ref[plane, rows], back_gain1, back_mean1)
            back = back - scaled(normal, back_normal1)
            valid = inv_ref[plane, rows] > 0.0
            dx_ref[plane, rows] = jnp.where(valid, dx_ref[plane, rows] + back, 0.0)
        return carry

    sweep(unnorm, 0)

    def give_back(plane, here, spot, there):
        image_ref[spot, there] = dx_ref[plane, here]

    image_ref[...] = jnp.zeros(image_ref.shape, f32)
    each_image(bucket_of, pair, give_back)

    for spot in range(2 * STRIPS):
        target = strip_place(pair, spot, strip_count)
        for within in range(SR):
            rows = slice(within * CW, within * CW + CW)
            payload_ref[target, within] = image_ref[spot, rows].astype(bf16)

    def finish():
        copy = pltpu.make_async_copy(payload_ref, payload_hbm, sem)
        copy.start()
        vector_ref[...] = flat_ref[...]
        for n in range(3):
            vector_ref[n : n + 1] = jnp.sum(acc_ref[n], axis=0, keepdims=True)
        copy.wait()

    if pairs == 1:
        finish()
    else:
        pl.when(pair == pairs - 1)(finish)


def run_exit(place, buckets, state, back, flat, vec, strip_count):
    pairs = strip_count // 8
    payload = (strip_count, SR, CW, C2)
    make = pltpu.VMEM if pairs == 1 else jax.ShapeDtypeStruct
    plane_f32 = pltpu.VMEM((4, AREA, C2), f32)
    arrays = [*state, *back]
    if pairs == 1:
        arrays = held_in(pltpu.VMEM, *arrays)
    return pl.pallas_call(
        functools.partial(exit_kernel, pairs, strip_count),
        grid=() if pairs == 1 else (pairs,),
        in_specs=[SMEM] * 2
        + pair_specs(pairs, STATE + BACK, pl.Buffered(1))
        + whole_specs(pairs, [flat.shape, vec.shape]),
        out_specs=[HBM] + whole_specs(pairs, [flat.shape]),
        out_shape=[pltpu.HBM(payload, bf16), make(flat.shape, f32)],
        scratch_shapes=[
            pltpu.VMEM(payload, bf16),
            pltpu.VMEM((2 * STRIPS, STRIP_ROWS, C2), f32),
            pltpu.VMEM((4, AREA + 2 * LINE, C2), f32),
            plane_f32,
            plane_f32,
            pltpu.VMEM((3, 8, C2), f32),
            pltpu.SemaphoreType.DMA,
        ],
        compiler_params=roomy(8 if pairs == 1 else 40),
        name="exit",
    )(place, buckets, *arrays, flat, vec)


def dense_blocks(values):
    return jnp.concatenate([values[:, :HALF], values[:, HALF:]], axis=2).astype(bf16)


def pack_kernel(master_ref, dense_ref):
    dense_ref[...] = dense_blocks(master_ref[...])


def pack(master):
    owned = master.shape[0]
    return pl.pallas_call(
        pack_kernel,
        out_shape=jax.ShapeDtypeStruct((owned, HALF, 2 * BS), bf16),
        name="pack",
    )(master)


def pack_pieces_kernel(place_ref, master_hbm, pixel_hbm, *refs):
    out_refs, (wide_ref, master_ref, pixel_ref, sem) = refs[:-4], refs[-4:]
    owned = master_ref.shape[0]
    slots = pixel_ref.shape[2]
    copies = [pltpu.make_async_copy(pixel_hbm, pixel_ref, sem.at[0])]
    parts = [(0, owned // 2), (owned // 2, owned - owned // 2)]
    for n, part in enumerate(parts):
        copies.append(
            pltpu.make_async_copy(
                master_hbm.at[pl.ds(*part)], master_ref.at[pl.ds(*part)], sem.at[1 + n]
            )
        )
    for copy in copies:
        copy.start()
    copies[0].wait()

    def widen_row(row, carry):
        start = pl.multiple_of(row * CW * slots, 8)
        values = pixel_ref[row].astype(f32).reshape(CW * slots, C2)
        wide_ref[pl.ds(start, CW * slots)] = values
        return carry

    lax.fori_loop(0, SR, widen_row, 0)
    for k, ref in enumerate(out_refs):
        for other in range(2):
            slot = place_ref[0] ^ (2 * k + other)
            first = other * (ref.shape[0] - STRIP_ROWS)
            strip = wide_ref[pl.ds(slot, STRIP_ROWS, stride=slots)]
            ref[first : first + STRIP_ROWS] = strip.astype(bf16)
    for (first, count), copy in zip(parts, copies[1:]):
        copy.wait()
        dense = dense_blocks(master_ref[first : first + count]).reshape(count * HALF, 2 * BS)
        start = STRIP_ROWS + first * HALF
        for ref in out_refs[:3]:
            ref[start : start + count * HALF] = dense


def pack_pieces(place, master, pixels):
    slots = pixels.shape[2]
    rows = master.shape[0] * HALF
    shapes = [(rows + 2 * STRIP_ROWS, 2 * BS)] * 3 + [(2 * STRIP_ROWS, 2 * BS)]
    return pl.pallas_call(
        pack_pieces_kernel,
        in_specs=[SMEM] + [HBM] * 2,
        out_specs=[VMEM_BLOCK] * 4,
        out_shape=[pltpu.VMEM(shape, bf16) for shape in shapes],
        scratch_shapes=[
            pltpu.VMEM((STRIP_ROWS * slots, C2), f32),
            pltpu.VMEM(master.shape, f32),
            pltpu.VMEM(pixels.shape, bf16),
            pltpu.SemaphoreType.DMA((3,)),
        ],
        compiler_params=roomy(12),
        name="pack",
    )(place, *held_in(pltpu.HBM, master, pixels))


def fold_pair_kernel(near_ref, got_ref, own_ref, *part_refs):
    share = own_ref.shape[0]

    def one(n, carry):
        own_ref[n] = near_ref[n].astype(f32) + got_ref[n].astype(f32)
        for k, ref in enumerate(part_refs):
            here = (k + 1) * share + n
            ref[n] = near_ref[here] + got_ref[here]
        return carry

    lax.fori_loop(0, share, one, 0, unroll=4)


def fold_pair(near, got, groups):
    shape = ((near.shape[0] - 1) // groups,) + near.shape[1:]
    return pl.pallas_call(
        fold_pair_kernel,
        in_specs=[VMEM_BLOCK] * 2,
        out_specs=[VMEM_BLOCK] * groups,
        out_shape=[pltpu.VMEM(shape, f32)] + [pltpu.VMEM(shape, bf16)] * (groups - 1),
        compiler_params=roomy(4),
        name="fold_pair",
    )(*held_in(pltpu.VMEM, near, got))


def fold_tile_kernel(pieces, spot_ref, *refs):
    piece_refs, refs = refs[:pieces], refs[pieces:]
    vector_refs, refs = refs[:pieces], refs[pieces:]
    out_refs, sum_ref = refs[:-1], refs[-1]
    groups = len(out_refs)
    share = out_refs[0].shape[0]
    owned = piece_refs[0].shape[0]
    total = vector_refs[0][...]
    for ref in vector_refs[1:]:
        total = total + ref[...]
    for n in range(sum_ref.shape[0]):
        sum_ref[n] = jnp.zeros((HALF, 128), f32)
    for n in range(VEC_BLOCKS):
        sum_ref[n] = total[n * HALF : (n + 1) * HALF]

    def one(n, carry):
        for k, out_ref in enumerate(out_refs):
            number = lax.rem(spot_ref[0] + k, groups) * share + n
            block = jnp.minimum(number, owned - 1)
            total = piece_refs[0][block].astype(f32)
            for ref in piece_refs[1:]:
                total = total + ref[block].astype(f32)
            rest = sum_ref[jnp.maximum(number - owned, 0)]
            out_ref[n] = jnp.where(number < owned, total, rest).astype(out_ref.dtype)
        return carry

    lax.fori_loop(0, share, one, 0, unroll=share <= 16)


def fold_tile(spot, pieces, vectors, extra, groups):
    shape = ((pieces[0].shape[0] + extra) // groups,) + pieces[0].shape[1:]
    return pl.pallas_call(
        functools.partial(fold_tile_kernel, len(pieces)),
        in_specs=[SMEM] + [VMEM_BLOCK] * (len(pieces) + len(vectors)),
        out_specs=[VMEM_BLOCK] * groups,
        out_shape=[pltpu.VMEM(shape, f32)] + [pltpu.VMEM(shape, bf16)] * (groups - 1),
        scratch_shapes=[pltpu.VMEM((extra, HALF, 128), f32)],
        compiler_params=roomy(8),
        name="fold_tile",
    )(spot, *held_in(pltpu.VMEM, *pieces, *vectors))


def fold_batch_kernel(owned, vector_weight, spot_ref, *refs):
    part_refs, (total_ref, norm_ref) = refs[:-2], refs[-2:]
    share = total_ref.shape[0]
    square = jnp.zeros((8, 128), f32)
    for n in range(share):
        total = part_refs[0][n].astype(f32)
        for ref in part_refs[1:]:
            total = total + ref[n].astype(f32)
        total_ref[n] = total.astype(bf16)
        weight = jnp.where(spot_ref[0] * share + n < owned, 1.0, vector_weight)
        square = square + weight * fold(total * total)
    square = jnp.sum(jnp.sum(square, axis=1, keepdims=True), axis=0, keepdims=True)
    norm_ref[...] = jnp.broadcast_to(square[None], norm_ref.shape)


def fold_batch(spot, parts, owned, tile_count):
    count = tile_count * len(parts)
    return pl.pallas_call(
        functools.partial(fold_batch_kernel, owned, 1.0 / tile_count),
        in_specs=[SMEM] + [VMEM_BLOCK] * len(parts),
        out_specs=[VMEM_BLOCK] * 2,
        out_shape=[pltpu.VMEM(parts[0].shape, bf16), pltpu.VMEM((count, 1, 128), f32)],
        name="fold_batch",
    )(spot, *held_in(pltpu.VMEM, *parts))


def update_kernel(owned, groups, spot_ref, norm_ref, *refs):
    quarters, refs = refs[:groups], refs[groups:]
    stat_hbm, out_hbm, (vector_ref, clip_ref), refs = refs[:5], refs[5:10], refs[10:12], refs[12:]
    stat_refs, out_refs, (in_sem, out_sem) = refs[:5], refs[5:10], refs[10:]
    master_ref, left_stat_ref, right_stat_ref, left_root_ref, right_root_ref = stat_refs
    grad_ref, left_ref, right_ref, new_ref, copy_ref = out_refs
    share = quarters[0].shape[0]
    spans = spans_of(owned)

    def copies_of(sources, targets, sems):
        return [
            [
                pltpu.make_async_copy(
                    source.at[pl.ds(*span)], target.at[pl.ds(*span)], sems.at[5 * n + k]
                )
                for k, (source, target) in enumerate(zip(sources, targets))
            ]
            for n, span in enumerate(spans)
        ]

    copies_in = copies_of(stat_hbm, stat_refs, in_sem)
    copies_out = copies_of(out_refs, out_hbm, out_sem)
    for copies in copies_in:
        for copy in copies:
            copy.start()
    norm = jnp.sqrt(jnp.sum(norm_ref[...], axis=0))
    factor = jnp.minimum(1.0, clip_limit / norm)
    left_half = lax.broadcasted_iota(jnp.int32, (HALF, 128), 1) < BS

    def summed(number):
        source = number // share
        local = number - source * share
        turn = lax.rem(spot_ref[0] - source + groups, groups)
        value = quarters[0][local].astype(f32)
        for k in range(1, groups):
            value = jnp.where(turn == k, quarters[k][local].astype(f32), value)
        return value * factor

    def side_by_side(first, count):
        sides = []
        for n in range(first, first + count, 2):
            dense = summed(n)
            turned = pltpu.roll(dense, BS, 1)
            if n + 1 < first + count:
                second = summed(n + 1)
                top = jnp.where(left_half, dense, pltpu.roll(second, BS, 1))
                low = jnp.where(left_half, turned, second)
                side = jnp.concatenate([top, low], axis=0)
                grad_ref[n + 1] = pltpu.roll(side, BS, 1)[:, :BS]
            else:
                side = jnp.concatenate([dense, turned], axis=0)[:, :BS]
            grad_ref[n] = side[:, :BS]
            sides.append(side.astype(bf16))
        return jnp.concatenate(sides, axis=1)

    def diagonal_of(count):
        order = (count * BS, count * BS)
        return lax.broadcasted_iota(jnp.int32, order, 0) // BS == (
            lax.broadcasted_iota(jnp.int32, order, 1) // BS
        )

    clip_ref[...] = norm
    for n in range(vector_ref.shape[0]):
        vector_ref[n] = summed(owned + n)
    for (first, length), arriving, leaving in zip(spans, copies_in, copies_out):
        parts = [(n, min(4, first + length - n)) for n in range(first, first + length, 4)]
        wides = [side_by_side(*part) for part in parts]
        tall = [
            jnp.where(diagonal_of(count), jnp.concatenate([wide] * count, axis=0), 0.0)
            for (_, count), wide in zip(parts, wides)
        ]
        lefts = [product_nt(one, wide) for one, wide in zip(tall, wides)]
        rights = [product_tn(wide, wide) for wide in wides]
        for copy in arriving:
            copy.wait()
        stepped = []
        for (start, count), wide in zip(parts, wides):
            roots = left_root_ref[pl.ds(start, count)].reshape(count * BS, BS).astype(bf16)
            stepped.append(product(roots, wide))
        for (start, count), left, right in zip(parts, lefts, rights):
            here = pl.ds(start, count)
            left_ref[here] = 0.5 * left_stat_ref[here] + 0.5 * left.reshape(count, BS, BS)
            for n in range(count):
                at = n // 2 * 128
                block = right[n * BS : n * BS + BS, at : min(at + 128, count * BS)]
                if n % 2:
                    block = pltpu.roll(block, BS, 1)
                right_ref[start + n] = 0.5 * right_stat_ref[start + n] + 0.5 * block[:, :BS]
        for (start, count), value in zip(parts, stepped):
            here = pl.ds(start, count)
            value = jnp.where(diagonal_of(count), value, 0.0).astype(bf16)
            roots = right_root_ref[here].reshape(count * BS, BS).astype(bf16)
            value = product(value, roots).reshape(count, BS, BS)
            new = master_ref[here] - rate_matrix * value
            new_ref[here] = new
            copy_ref[here] = new.astype(bf16)
        for copy in leaving:
            copy.start()
    for leaving in copies_out:
        for copy in leaving:
            copy.wait()


def spans_of(owned):
    spans = []
    first = 0
    while first < owned:
        length = min(8 if first == 0 else 12, owned - first)
        spans.append((first, length))
        first += length
    return spans


def update(spot, norm, quarters, extra, *stats):
    shape = stats[0].shape
    groups = len(quarters)
    types = [f32] * 4 + [bf16]
    steps = len(spans_of(shape[0]))
    return pl.pallas_call(
        functools.partial(update_kernel, shape[0], groups),
        in_specs=[SMEM] + [VMEM_BLOCK] * (groups + 1) + [HBM] * 5,
        out_specs=[HBM] * 5 + [VMEM_BLOCK] * 2,
        out_shape=[pltpu.HBM(shape, kind) for kind in types]
        + [
            pltpu.VMEM((extra, HALF, 128), f32),
            pltpu.VMEM((1, 128), f32),
        ],
        scratch_shapes=[pltpu.VMEM(shape, f32)] * 5
        + [pltpu.VMEM(shape, kind) for kind in types]
        + [
            pltpu.SemaphoreType.DMA((5 * steps,)),
            pltpu.SemaphoreType.DMA((5 * steps,)),
        ],
        compiler_params=roomy(20),
        name="update",
    )(spot, *held_in(pltpu.VMEM, norm, *quarters), *held_in(pltpu.HBM, *stats))


def share_out(pieces, axis):
    return lax.all_to_all(pieces, axis, split_axis=0, concat_axis=0, tiled=True)


def swap(piece, distance):
    count = lax.axis_size("tile")
    return lax.ppermute(piece, "tile", [(i, i ^ distance) for i in range(count)])


def on_device(
    pixels,
    buckets,
    slot_owner_table,
    out_grad,
    master,
    left_stat,
    right_stat,
    left_root,
    right_root,
    vectors,
    moment,
):
    tile_count = lax.axis_size("tile")
    tile_place = lax.axis_index("tile")
    slot_count = pixels.shape[2]
    group_count = tile_count // STRIPS
    pairs = group_count // 2
    owned = master.shape[0]
    slots = owned * tile_count
    batch_count = lax.axis_size("batch")
    spot = lax.axis_index("batch").astype(jnp.int32).reshape(1)
    extra = extra_of(owned, batch_count)
    place = tile_place.astype(jnp.int32).reshape(1)
    paired = tile_count == 8
    numbers = jnp.arange(slots, dtype=jnp.int32)
    slot_of = jnp.sum(
        jnp.where(slot_owner_table[None, :] == numbers[:, None], numbers[None, :], 0), axis=1
    )
    if paired:
        owner = slot_of // owned
        apart = owner ^ tile_place
        apart = (apart & 1) * (tile_count // 2) + (apart >> 1)
        slot_of = slot_of + owned * (apart - owner)
    half = slots // 2
    near_place = jnp.where(slot_of < half, slot_of, half)
    far_place = jnp.where(slot_of < half, half, slot_of - half)
    vec = vectors.reshape(-1, 128)
    turned = lax.dynamic_index_in_dim(
        buckets.reshape(group_count, slot_count), tile_place, 1, keepdims=False
    ) >= 2
    flips = turned.reshape(-1, 1, 1, 1)
    goal = out_grad.reshape(2 * pairs, H3, W3, C3)
    goal = jnp.where(flips, goal.transpose(0, 2, 1, 3), goal)[:, :LINES]
    goal = goal.reshape(pairs, 2, LINES, W3, C3).transpose(0, 2, 3, 1, 4)
    goal = goal.reshape(pairs, LINES, 2 * W3, C3)
    goal = jnp.pad(goal, ((0, 0), (0, 0), (0, LINE - 2 * W3), (0, WIDE - C3)))
    goal = goal.reshape(pairs, AREA, WIDE)

    if paired:
        own, for_x, for_y, for_both = pack_pieces(
            place, master, pixels[0, 0].transpose(1, 2, 0, 3)
        )
        goal, vec, slot_of, near_place, far_place, for_both = lax.optimization_barrier(
            (goal, vec, slot_of, near_place, far_place, for_both)
        )
        from_x, from_y, strips_both = swap(for_x, 2), swap(for_y, 4), swap(for_both, 6)
        near_half = (owned + 1) // 2
        middle = STRIP_ROWS + near_half * HALF
        first_half = swap(from_x[STRIP_ROWS:middle], 4)
        second_half = swap(from_y[middle : STRIP_ROWS + owned * HALF], 2)
        mine = [own, from_x, from_y, strips_both, first_half, second_half]
        both = mine + [swap(piece, 1) for piece in mine]
        strips = both[:4] + both[6:10]
        pieces = [both[n] for n in (0, 1, 2, 4, 5, 6, 7, 8, 10, 11)]
        spans = [(STRIP_ROWS, owned)] * 3 + [(0, near_half), (0, owned - near_half)]
        spans = spans * 2
    else:
        pieces = [lax.all_gather(pack(master), "tile", axis=0, tiled=True).reshape(-1, 2 * BS)]
        spans = [(0, slots)]
        strips = share_out(pixels.reshape(tile_count, STRIP, C2), "tile")
        strips = [jnp.pad(strips, ((0, 0), (0, STRIP_ROWS - STRIP), (0, 0)))]

    weights = run_unpack(slot_of, pieces, spans)
    state = run_entry(place, buckets, strips, vec, tile_count)
    result, *back, near, far, flat = run_main(
        (near_place, far_place),
        place,
        buckets,
        state,
        goal,
        vec,
        weights,
        tile_count,
    )
    pixel_back, vector = run_exit(place, buckets, state, back, flat, vec, tile_count)
    if paired:
        own, *parts = fold_pair(near, swap(far, 1), tile_count // 2)
        pieces = [own] + [swap(part, 2 * k + 2) for k, part in enumerate(parts)]
        vector, _ = lax.optimization_barrier((vector, parts[0]))
        vector = vector + swap(vector, 1)
        vectors_in = [vector] + [swap(vector, 2 * k) for k in range(1, tile_count // 2)]
    else:
        outgoing = jnp.concatenate([near[:half], far[:half]], axis=0)
        pieces = list(share_out(outgoing.reshape(tile_count, owned, HALF, 128), "tile"))
        vectors_in = list(lax.all_gather(vector, "tile"))
    result, pieces[1] = lax.optimization_barrier((result, pieces[1]))
    result = result.reshape(pairs, LINES, LINE, WIDE)[:, :, : 2 * W3, :C3]
    result = result.reshape(pairs, LINES, W3, 2, C3).transpose(0, 3, 1, 2, 4)
    result = result.reshape(2 * pairs, LINES, W3, C3)
    result = jnp.pad(result, ((0, 0), (0, H3 - LINES), (0, 0), (0, 0)))
    result = jnp.where(flips, result.transpose(0, 2, 1, 3), result)
    result = result.reshape(out_grad.shape)
    result = with_layout_constraint(result, Layout(major_to_minor=(0, 1, 2, 4, 5, 3, 6)))
    result, vectors_in[0] = lax.optimization_barrier((result, vectors_in[0]))
    own, *parts = fold_tile(spot, pieces, vectors_in, extra, batch_count)
    pixel_back, parts[0] = lax.optimization_barrier((pixel_back, parts[0]))
    returned = share_out(pixel_back, "tile")
    parts = [
        lax.ppermute(part, "batch", [(i, (i + k + 1) % batch_count) for i in range(batch_count)])
        for k, part in enumerate(parts)
    ]
    quarter, norm = fold_batch(spot, [own] + parts, owned, tile_count)
    returned, norm = lax.optimization_barrier((returned, norm))
    norm = share_out(norm, ("batch", "tile"))
    returned = returned.astype(f32).reshape(pixels.shape)
    returned = with_layout_constraint(returned, Layout(major_to_minor=(0, 1, 3, 4, 2, 5)))
    returned, norm = lax.optimization_barrier((returned, norm))
    quarters = [quarter] + [
        lax.ppermute(quarter, "batch", [(i, (i + k) % batch_count) for i in range(batch_count)])
        for k in range(1, batch_count)
    ]
    block_grad, left_new, right_new, master_new, weight_copy, whole_vector, clip = update(
        spot, norm, quarters, extra, master, left_stat, right_stat, left_root, right_root
    )
    clip_norm = clip[0, 0]
    share = vectors.shape[0] // tile_count
    whole_vector = whole_vector.reshape(-1)
    vec_grad = lax.dynamic_slice_in_dim(whole_vector, tile_place * share, share, 0)
    vec_moment = moment + vec_grad * vec_grad
    own_vectors = lax.dynamic_slice_in_dim(vectors, tile_place * share, share, 0)
    vec_new = own_vectors - rate_vector * vec_grad / (jnp.sqrt(vec_moment) + eps_adagrad)
    return (
        result,
        returned,
        clip_norm,
        block_grad,
        left_new,
        right_new,
        master_new,
        weight_copy,
        vec_grad,
        vec_moment,
        vec_new,
    )


def solution(mesh):
    placed = (
        P("batch", "tile", None, None, None, None),
        P("batch"),
        P(),
        P("batch", "tile", None, None, None, None, None),
        P("tile", None, None),
        P("tile", None, None),
        P("tile", None, None),
        P("tile", None, None),
        P("tile", None, None),
        P(),
        P("tile"),
    )
    return jax.shard_map(
        on_device,
        mesh=mesh,
        in_specs=placed,
        out_specs=(
            P("batch", "tile", None, None, None, None, None),
            P("batch", "tile", None, None, None, None),
            P(),
            P("tile", None, None),
            P("tile", None, None),
            P("tile", None, None),
            P("tile", None, None),
            P("tile", None, None),
            P("tile"),
            P("tile"),
            P("tile"),
        ),
        check_vma=False,
    )
```

```python
import functools

import jax
import jax.numpy as jnp
from jax import lax
from jax.experimental import pallas as pl
from jax.experimental.layout import Layout, with_layout_constraint
from jax.experimental.pallas import tpu as pltpu
from jax.sharding import PartitionSpec as P

C2 = 128
HID2 = 512
C3 = 320
HID3 = 1280
CH = 36
CW = 36
STRIPS = 4
BS = 64
SR = CH // STRIPS
H3 = CH // 2
W3 = CW // 2
LONG = 7 * CH // 9
LINES = LONG // 2
WIDE = 384
LINE = 40
AREA = LINES * LINE
STEP = 2 * LINE
STEPS = AREA // STEP
HALF = BS // 2
STRIP = SR * CW
STRIP_ROWS = STRIP + -STRIP % 16

eps_norm = 1e-05
clip_limit = 1.0
rate_matrix = 0.3
rate_vector = 0.3
eps_adagrad = 1e-08
f32 = jnp.float32
bf16 = jnp.bfloat16

SHAPES = [(C2, HID2), (HID2, C2), (9 * C2, C3), (C3, HID3), (HID3, C3)]
USED = sum(rows // BS * (cols // BS) for rows, cols in SHAPES)
VEC_ROWS = (6 * C2 + HID2 + C2 + C3 + 6 * C3 + HID3 + C3) // 128


VEC_BLOCKS = -(-VEC_ROWS // HALF)
VEC_SENT = VEC_ROWS + -VEC_ROWS % 16


def extra_of(owned, groups):
    return VEC_BLOCKS + -(owned + VEC_BLOCKS) % groups


def product(left, right):
    return jnp.dot(left, right, preferred_element_type=f32)


def product_nt(left, right):
    return lax.dot_general(left, right, (((1,), (1,)), ((), ())), preferred_element_type=f32)


def product_tn(left, right):
    return lax.dot_general(left, right, (((0,), (0,)), ((), ())), preferred_element_type=f32)


def gelu_pair(values):
    bell = jnp.exp2(values * values * (-0.5 * 1.4426950408889634))
    step = pl.reciprocal(1.0 + (0.3275911 * 0.7071067811865476) * jnp.abs(values), approx=True)
    tail = step * (
        0.5 * 0.254829592
        + step
        * (
            0.5 * -0.284496736
            + step
            * (0.5 * 1.421413741 + step * (0.5 * -1.453152027 + step * (0.5 * 1.061405429)))
        )
    )
    tail = tail * bell
    share = jnp.where(values >= 0.0, 1.0 - tail, tail)
    return (values * share, share + values * (bell * 0.3989422804014327))


def fold(values):
    chans = values.shape[-1]
    return jnp.sum(values.reshape(-1, 8, chans), axis=0)


def by_image(total):
    total = total + pltpu.roll(total, 4, 0)
    total = total + pltpu.roll(total, 2, 0)
    return jnp.sum(total, axis=1, keepdims=True)


def line(pattern):
    return jnp.concatenate([pattern] * (LINE // 8), axis=0)


def spread(pattern, chans):
    return jnp.broadcast_to(pattern, (8, chans))


def affine(values, factor, shift):
    tiles = values.reshape(-1, 8, values.shape[-1])
    return (tiles * factor + shift).reshape(values.shape)


def scaled(values, factor):
    tiles = values.reshape(-1, 8, values.shape[-1])
    return (tiles * factor).reshape(values.shape)


def from_left(values):
    return pltpu.roll(values, 2, 0)


def from_right(values):
    return pltpu.roll(values, values.shape[0] - 2, 0)


def rounded(values):
    return values.astype(bf16).astype(f32)


def widen(values):
    return jnp.concatenate([values] * (WIDE // 128), axis=-1)


def norm_terms(total, square, count):
    mean = by_image(total) / count
    scaling = lax.rsqrt(by_image(square) / count - mean * mean + eps_norm)
    return (mean, scaling)


def sweep(visit, start):
    return lax.fori_loop(0, STEPS, visit, start, unroll=True)


def step_rows(k, lines=0):
    start = k * STEP + lines * LINE
    return pl.ds(start if isinstance(k, int) else pl.multiple_of(start, LINE), STEP)


def held_in(space, *arrays):
    return [pltpu.with_memory_space_constraint(array, space) for array in arrays]


VMEM_BLOCK = pl.BlockSpec(memory_space=pltpu.VMEM)
HBM = pl.BlockSpec(memory_space=pltpu.HBM)
SMEM = pl.BlockSpec(memory_space=pltpu.SMEM)


def roomy(mebibytes):
    return pltpu.CompilerParams(vmem_limit_bytes=mebibytes * 1024 * 1024)


def image_shape(bucket_of, pair, image):
    bucket = bucket_of(2 * pair + image)
    plain = jnp.where(bucket == 0, 5 * CH // 9, 7 * CH // 9)
    across = jnp.where(bucket == 0, CW, 7 * CW // 9)
    turned = (bucket >= 2).astype(jnp.int32)
    return (
        jnp.where(turned > 0, 5 * CW // 9, plain),
        jnp.where(turned > 0, CH, across),
        turned,
    )


def bucket_reader(place_ref, bucket_ref, strip_count):
    return lambda group: bucket_ref[group * strip_count + place_ref[0]]


class Geometry:
    def __init__(self, bucket_of, pair):
        parity = lax.broadcasted_iota(jnp.int32, (8, 128), 0) % 2
        even, odd = (image_shape(bucket_of, pair, image) for image in range(2))
        high, broad, turned = (jnp.where(parity == 0, a, b) for a, b in zip(even, odd))
        self.high = high
        self.count_two = (high * broad * C2).astype(f32)[:, :1]
        self.high3 = (high + 1) // 2
        broad3 = (broad + 1) // 2
        self.count_three = (self.high3 * broad3 * C3).astype(f32)[:, :1]
        place = lax.broadcasted_iota(jnp.int32, (LINE, 128), 0) // 2
        inside = lax.broadcasted_iota(jnp.int32, (LINE, 128), 0) < 2 * W3
        self.reach = []
        self.col_share = []
        for pc in range(2):
            column = 2 * place + pc
            self.reach.append(jnp.where(inside & (column < line(broad)), line(high), 0))
            edge = (column == 0) | (column == line(broad) - 1)
            self.col_share.append(jnp.where(edge, 0.5, 1.0 / 3.0))
        self.reach3 = jnp.where(inside & (place < line(broad3)), line(self.high3), 0)
        edge3 = (place == 0) | (place == line(broad3) - 1)
        self.col_share3 = jnp.where(edge3, 0.5, 1.0 / 3.0)
        self.flipped = jnp.concatenate([turned] * (STEP // 8), axis=0) > 0

    def share(self, plane, k):
        pr, pc = plane // 2, plane % 2
        return self.lines(4 * k + pr, 2, self.reach[pc], self.col_share[pc], self.high)

    def share3(self, k):
        return self.lines(2 * k, 1, self.reach3, self.col_share3, self.high3)

    def lines(self, row, stride, reach, col_share, height):
        parts = []
        for n in range(2):
            here = row + stride * n
            row_share = jnp.where((here == 0) | (here == height - 1), 0.5, 1.0 / 3.0)
            parts.append(jnp.where(here < reach, line(row_share) * col_share, 0.0))
        return jnp.concatenate(parts, axis=0)


def strip_place(pair, spot, strip_count):
    return lax.rem(pair * 8 + strip_count - 2 + spot, strip_count)


def each_image(bucket_of, pair, visit):
    for image in range(2):
        way = image_shape(bucket_of, pair, image)[2]

        @pl.when(way == 0)
        def _():
            def one(r, carry):
                for plane in range(4):
                    row = 2 * r + plane // 2
                    strip = row // SR
                    there = pl.ds((row - strip * SR) * CW + plane % 2, W3, stride=2)
                    here = pl.ds(r * LINE + image, W3, stride=2)
                    visit(plane, here, image * STRIPS + strip, there)
                return carry

            lax.fori_loop(0, LINES, one, 0)

        @pl.when(way == 1)
        def _():
            def one(r, carry):
                for plane in range(4):
                    for strip in range(STRIPS):
                        first = (plane % 2 + strip * SR) % 2
                        count = (SR - first + 1) // 2
                        done = (strip * SR + first) // 2
                        column = 2 * r + plane // 2
                        there = pl.ds(first * CW + column, count, stride=2 * CW)
                        here = pl.ds(r * LINE + image + 2 * done, count, stride=2)
                        visit(plane, here, image * STRIPS + strip, there)
                return carry

            lax.fori_loop(0, LINES, one, 0)


def row_windows(col_ref, pc, k):
    both = col_ref[pc, step_rows(k, 1)] + col_ref[2 + pc, step_rows(k, 1)]
    return (both + col_ref[2 + pc, step_rows(k)], both + col_ref[pc, step_rows(k, 2)])


def put_col_windows(col_ref, pr, k, even, odd):
    both = even + odd
    col_ref[pr * 2, step_rows(k, 1)] = both + from_left(odd)
    col_ref[pr * 2 + 1, step_rows(k, 1)] = both + from_right(even)


def clear_edges(col_ref):
    zero_line = jnp.zeros((LINE, C2), f32)
    for plane in range(4):
        col_ref[plane, 0:LINE] = zero_line
        col_ref[plane, AREA + LINE : AREA + 2 * LINE] = zero_line


def entry_kernel(pairs, strip_count, piece_count, place_ref, bucket_ref, vec_ref, *refs):
    piece_refs, refs = refs[:piece_count], refs[piece_count:]
    x_out, inv_out, pool_out, mix_out, stat_out, image_ref, col_ref = refs
    pair = pl.program_id(0) if pairs > 1 else 0
    x_ref, inv_ref, pool_ref, mix_ref = (ref.at[0] for ref in (x_out, inv_out, pool_out, mix_out))
    bucket_of = bucket_reader(place_ref, bucket_ref, strip_count)
    shape = Geometry(bucket_of, pair)
    gain1, bias1, scale1 = (vec_ref[n : n + 1] for n in range(3))
    clear_edges(col_ref)
    if piece_count > 1:
        half = piece_count // 2
        for n, ref in enumerate(piece_refs):
            source = place_ref[0] ^ (n // half + 2 * (n % half))
            spot = lax.rem(source + 2, 2 * STRIPS)
            first = 0 if n < half else ref.shape[0] - STRIP_ROWS
            image_ref[spot] = ref[first : first + STRIP_ROWS].astype(f32)
    else:
        for spot in range(2 * STRIPS):
            source = strip_place(pair, spot, strip_count)
            image_ref[spot] = piece_refs[0][source].astype(f32)

    def take_in(plane, here, spot, there):
        x_ref[plane, here] = image_ref[spot, there]

    each_image(bucket_of, pair, take_in)

    def arrange(k, carry):
        total, square = carry
        rows = step_rows(k)
        for plane in range(4):
            share = shape.share(plane, k)
            inv_ref[plane, rows] = share
            values = jnp.where(share > 0.0, x_ref[plane, rows], 0.0)
            x_ref[plane, rows] = values
            total = total + fold(values)
            square = square + fold(values * values)
        return (total, square)

    nothing = jnp.zeros((8, C2), f32)
    total, square = sweep(arrange, (nothing, nothing))
    mean1, scaling1 = norm_terms(total, square, shape.count_two)
    factor1 = scaling1 * gain1
    shift1 = bias1 - mean1 * scaling1 * gain1

    def window_cols(k, carry):
        rows = step_rows(k)
        for pr in range(2):
            masked = []
            for pc in range(2):
                plane = pr * 2 + pc
                normal = rounded(affine(x_ref[plane, rows], factor1, shift1))
                masked.append(jnp.where(inv_ref[plane, rows] > 0.0, normal, 0.0))
            put_col_windows(col_ref, pr, k, *masked)
        return carry

    sweep(window_cols, 0)

    def mix(k, carry):
        total, square = carry
        rows = step_rows(k)
        for pc in range(2):
            windows = row_windows(col_ref, pc, k)
            for pr in range(2):
                plane = pr * 2 + pc
                values = x_ref[plane, rows]
                share = inv_ref[plane, rows]
                pooled = windows[pr] * share - rounded(affine(values, factor1, shift1))
                pooled = jnp.where(share > 0.0, pooled, 0.0)
                mixed = values + scale1 * pooled
                pool_ref[plane, rows] = pooled
                mix_ref[plane, rows] = mixed
                total = total + fold(mixed)
                square = square + fold(mixed * mixed)
        return (total, square)

    total, square = sweep(mix, (nothing, nothing))
    mean2, scaling2 = norm_terms(total, square, shape.count_two)
    for n, value in enumerate((mean1, scaling1, mean2, scaling2)):
        stat_out[0, n] = spread(value, 128)


def pair_specs(pairs, shapes, mode=None):
    if pairs == 1:
        return [VMEM_BLOCK] * len(shapes)
    return [
        pl.BlockSpec(
            (1,) + shape, lambda t, rank=len(shape): (t,) + (0,) * rank, pipeline_mode=mode
        )
        for shape in shapes
    ]


def whole_specs(pairs, shapes):
    if pairs == 1:
        return [VMEM_BLOCK] * len(shapes)
    return [
        pl.BlockSpec(
            shape,
            lambda t, rank=len(shape): (0,) * rank,
            pipeline_mode=pl.Buffered(1),
        )
        for shape in shapes
    ]


def pair_arrays(pairs, shapes, kinds):
    make = pltpu.VMEM if pairs == 1 else jax.ShapeDtypeStruct
    return [make((pairs,) + shape, kind) for shape, kind in zip(shapes, kinds)]


STATE = [(4, AREA, C2)] * 4 + [(4, 8, 128)]
BACK = [(4, AREA, C2)] * 2 + [(2, 8, 128)]


def run_entry(place, buckets, pieces, vec, strip_count):
    pairs = strip_count // 8
    if pairs == 1:
        pieces = held_in(pltpu.VMEM, *pieces)
    return pl.pallas_call(
        functools.partial(entry_kernel, pairs, strip_count, len(pieces)),
        grid=() if pairs == 1 else (pairs,),
        in_specs=[SMEM] * 2 + whole_specs(pairs, [array.shape for array in (vec, *pieces)]),
        out_specs=pair_specs(pairs, STATE),
        out_shape=pair_arrays(pairs, STATE, [f32] * 5),
        scratch_shapes=[
            pltpu.VMEM((2 * STRIPS, STRIP_ROWS, C2), f32),
            pltpu.VMEM((4, AREA + 2 * LINE, C2), f32),
        ],
        compiler_params=roomy(6 if pairs == 1 else 40),
        name="entry",
    )(place, buckets, vec, *pieces)


WEIGHTS = [(C2, HID2), (HID2, C2), (9 * C2, WIDE), (WIDE, HID3), (HID3, WIDE)]


def unpack_kernel(spans, slot_ref, *refs):
    piece_refs, refs = refs[: len(spans)], refs[len(spans) :]
    weights, gathered_ref = refs[:-1], refs[-1]
    done = 0
    for ref, (first, count) in zip(piece_refs, spans):
        blocks = ref[first : first + count * HALF].reshape(count, HALF, 128)
        gathered_ref[done : done + count] = blocks
        done += count
    left_half = lax.broadcasted_iota(jnp.int32, (HALF, 128), 1) < BS
    offset = 0
    for (rows, cols), ref in zip(SHAPES, weights):
        wide = cols // BS
        for rb in range(rows // BS):
            for cb in range(0, wide, 2):
                number = offset + rb * wide + cb
                first = gathered_ref[slot_ref[number]]
                turned = pltpu.roll(first, BS, 1)
                if cb + 1 < wide:
                    second = gathered_ref[slot_ref[number + 1]]
                    top = jnp.where(left_half, first, pltpu.roll(second, BS, 1))
                    low = jnp.where(left_half, turned, second)
                else:
                    top = jnp.where(left_half, first, 0.0)
                    low = jnp.where(left_half, turned, 0.0)
                place = slice(cb * BS, cb * BS + 128)
                ref[rb * BS : rb * BS + HALF, place] = top
                ref[rb * BS + HALF : rb * BS + BS, place] = low
        offset += rows // BS * wide
    weights[3][C3:, :] = jnp.zeros((WIDE - C3, HID3), bf16)


def run_unpack(slot_of, pieces, spans):
    slots = slot_of.shape[0]
    return pl.pallas_call(
        functools.partial(unpack_kernel, spans),
        in_specs=[SMEM] + [VMEM_BLOCK] * len(pieces),
        out_specs=[VMEM_BLOCK] * 5,
        out_shape=[pltpu.VMEM(shape, bf16) for shape in WEIGHTS],
        scratch_shapes=[pltpu.VMEM((slots, HALF, 128), bf16)],
        compiler_params=roomy(6),
        name="unpack",
    )(slot_of, *held_in(pltpu.VMEM, *pieces))


def main_kernel(
    pairs,
    strip_count,
    slots,
    near_place,
    far_place,
    place_ref,
    bucket_ref,
    inv_in,
    mix_in,
    stat_in,
    goal_ref,
    vec_ref,
    w1_ref,
    w2_ref,
    we_ref,
    w3_ref,
    w4_ref,
    result_ref,
    zed_out,
    dx_out,
    mean_out,
    near_ref,
    far_ref,
    flat_ref,
    zed_ref,
    hid_ref,
    u_ref,
    g_ref,
    h_ref,
    dy_ref,
    patch_ref,
    dpatch_ref,
    inv3_ref,
    e_ref,
    col3_ref,
    pool3_ref,
    mix3_ref,
    dx3_ref,
    hid3_ref,
    dhid3_ref,
    u3_ref,
    g3_ref,
    h3_ref,
    dy3_ref,
    dpre_ref,
    gw1_ref,
    gw2_ref,
    gwe_ref,
    gw3_ref,
    gw4_ref,
    acc_two,
    acc_hid_two,
    acc_three,
    acc_hid_three,
):
    pair = pl.program_id(0) if pairs > 1 else 0
    grads = [gw1_ref, gw2_ref, gwe_ref, gw3_ref, gw4_ref]
    inv_ref, mix_ref, stat_ref = (ref.at[0] for ref in (inv_in, mix_in, stat_in))
    back_ref, dx_ref = zed_out.at[0], dx_out.at[0]
    left_half = lax.broadcasted_iota(jnp.int32, (HALF, 128), 1) < BS

    def at_pair(number, act):
        if pairs == 1:
            act()
        else:
            pl.when(pair == number)(act)

    def begin():
        acc_two[...] = jnp.zeros(acc_two.shape, f32)
        acc_hid_two[...] = jnp.zeros(acc_hid_two.shape, f32)
        acc_three[...] = jnp.zeros(acc_three.shape, f32)
        acc_hid_three[...] = jnp.zeros(acc_hid_three.shape, f32)

    at_pair(0, begin)
    shape = Geometry(bucket_reader(place_ref, bucket_ref, strip_count), pair)
    count_two, count_three, flipped = shape.count_two, shape.count_three, shape.flipped
    nothing = jnp.zeros((8, C2), f32)
    nothing3 = jnp.zeros((8, WIDE), f32)

    def vector_row(at, length):
        first, shift = at // 128, at % 128
        count = -(-(shift + length) // 128)
        row = jnp.concatenate([vec_ref[first + n : first + n + 1] for n in range(count)], axis=1)
        if shift:
            row = pltpu.roll(jnp.broadcast_to(row, (8, count * 128)), count * 128 - shift, 1)[:1]
        return row

    def wide_row(at):
        lane = lax.broadcasted_iota(jnp.int32, (1, WIDE), 1)
        return jnp.where(lane < C3, vector_row(at, C3)[:, :WIDE], 0.0)

    gain2, bias2, scale2 = (vec_ref[n : n + 1] for n in range(3, 6))
    hid_bias = vector_row(6 * C2, HID2)
    out_bias = vector_row(6 * C2 + HID2, C2)
    two = 7 * C2 + HID2
    embed_bias, gain3, bias3, scale3 = (wide_row(two + n * C3) for n in range(4))
    gain4, bias4, scale4 = (wide_row(two + n * C3) for n in range(4, 7))
    hid_bias3 = vector_row(two + 7 * C3, HID3)[:, :HID3]
    out_bias3 = wide_row(two + 7 * C3 + HID3)
    mean2, scaling2 = stat_ref[2], stat_ref[3]
    factor2 = scaling2 * gain2
    shift2 = bias2 - mean2 * scaling2 * gain2
    for plane in range(4):
        zed_ref[plane, 0:LINE] = jnp.zeros((LINE, C2), f32)
    col3_ref[0:LINE] = jnp.zeros((LINE, WIDE), f32)
    col3_ref[AREA + LINE : AREA + 2 * LINE] = jnp.zeros((LINE, WIDE), f32)

    def put_block(number, block):
        near_ref[near_place[number]] = block
        far_ref[far_place[number]] = block

    offsets = [0]
    for rows, cols in SHAPES:
        offsets.append(offsets[-1] + rows // BS * (cols // BS))

    def pack_part(which, values, row=0, col=0):
        rows, cols = SHAPES[which]
        wide = cols // BS
        values = values.astype(bf16)
        for rb in range(row // BS, min(rows, row + values.shape[0]) // BS):
            for cb in range(col // BS, min(cols, col + values.shape[1]) // BS, 2):
                number = offsets[which] + rb * wide + cb
                start = rb * BS - row
                at = slice(cb * BS - col, cb * BS - col + 128)
                top = values[start : start + HALF, at]
                low = values[start + HALF : start + BS, at]
                put_block(number, jnp.where(left_half, top, pltpu.roll(low, BS, 1)))
                if cb + 1 < wide:
                    put_block(number + 1, jnp.where(left_half, pltpu.roll(top, BS, 1), low))

    def plane_rows(plane):
        return slice(plane * AREA, plane * AREA + AREA)

    def begin_plane(plane):
        low = affine(mix_ref[plane], factor2, shift2).astype(bf16)
        h_ref[plane_rows(plane)] = low
        hid_ref[plane % 2] = product(low, w1_ref[...])

    begin_plane(0)
    for plane in range(4):
        if plane < 3:
            begin_plane(plane + 1)
        for k in range(STEPS):
            rows = step_rows(k)
            flat = slice(plane * AREA + k * STEP, plane * AREA + k * STEP + STEP)
            for at in range(0, HID2, 128):
                lanes = slice(at, at + 128)
                active, slope = gelu_pair(hid_ref[plane % 2, rows, lanes] + hid_bias[:, lanes])
                u_ref[flat, lanes] = active.astype(bf16)
                g_ref[flat, lanes] = slope.astype(bf16)
        out = product(u_ref[plane_rows(plane)], w2_ref[...]) + out_bias
        zed = jnp.where(inv_ref[plane] > 0.0, mix_ref[plane] + scale2 * out, 0.0)
        zed_ref[plane, LINE : LINE + AREA] = rounded(zed)

    def patches(k, carry):
        rows = step_rows(k)
        taps = []
        for ky in range(3):
            pr = (0 if ky == 1 else 1) * 2
            source = step_rows(k, 0 if ky == 0 else 1)
            even = zed_ref[pr, source]
            odd = zed_ref[pr + 1, source]
            taps.append((from_left(odd), even, odd))
        for ky in range(3):
            for kx in range(3):
                at = (3 * ky + kx) * C2
                tap = taps[ky][kx]
                if ky != kx:
                    tap = jnp.where(flipped, taps[kx][ky], tap)
                patch_ref[rows, at : at + C2] = tap.astype(bf16)
        return carry

    sweep(patches, 0)
    e_ref[...] = product(patch_ref[...], we_ref[...])

    def embed(k, carry):
        total, square = carry
        rows = step_rows(k)
        share = shape.share3(k)
        inv3_ref[rows] = share
        out = jnp.where(widen(share) > 0.0, e_ref[rows] + embed_bias, 0.0)
        e_ref[rows] = out
        return (total + fold(out), square + fold(out * out))

    total, square = sweep(embed, (nothing3, nothing3))
    mean3, scaling3 = norm_terms(total, square, count_three)
    factor3 = scaling3 * gain3
    shift3 = bias3 - mean3 * scaling3 * gain3

    def window_cols3(k, carry):
        rows = step_rows(k)
        normal = rounded(affine(e_ref[rows], factor3, shift3))
        masked = jnp.where(widen(inv3_ref[rows]) > 0.0, normal, 0.0)
        col3_ref[step_rows(k, 1)] = masked + from_left(masked) + from_right(masked)
        return carry

    sweep(window_cols3, 0)

    def row_windows3(k):
        return col3_ref[step_rows(k)] + col3_ref[step_rows(k, 1)] + col3_ref[step_rows(k, 2)]

    def mix3(k, carry):
        total, square = carry
        rows = step_rows(k)
        values = e_ref[rows]
        share = widen(inv3_ref[rows])
        pooled = row_windows3(k) * share - rounded(affine(values, factor3, shift3))
        pooled = jnp.where(share > 0.0, pooled, 0.0)
        mixed = values + scale3 * pooled
        pool3_ref[rows] = pooled
        mix3_ref[rows] = mixed
        return (total + fold(mixed), square + fold(mixed * mixed))

    total, square = sweep(mix3, (nothing3, nothing3))
    mean4, scaling4 = norm_terms(total, square, count_three)
    factor4 = scaling4 * gain4
    shift4 = bias4 - mean4 * scaling4 * gain4
    normal4 = (spread(scaling4, WIDE), spread(-mean4 * scaling4, WIDE))

    def prepare3(k, d_bias):
        rows = step_rows(k)
        h3_ref[rows] = affine(mix3_ref[rows], factor4, shift4).astype(bf16)
        goal = goal_ref[0, rows].astype(f32)
        goal = jnp.where(widen(inv3_ref[rows]) > 0.0, goal, 0.0)
        goal = scale4 * goal
        dy3_ref[rows] = goal.astype(bf16)
        return d_bias + fold(goal)

    acc_three[7] += sweep(prepare3, nothing3)

    def keep(which, value, row=0, col=0):
        if pairs == 1:
            pack_part(which, value, row, col)
        else:
            ref = grads[which]
            place = (slice(row, row + value.shape[0]), slice(col, col + value.shape[1]))

            @pl.when(pair == 0)
            def _():
                ref[place] = value

            @pl.when(pair > 0)
            def _():
                ref[place] += value

    def begin_chunk(at):
        lanes = slice(at, at + 256)
        hid3_ref[:, lanes] = product(h3_ref[...], w3_ref[:, lanes])
        dhid3_ref[:, lanes] = product_nt(dy3_ref[...], w4_ref[lanes])

    begin_chunk(0)
    for at in range(0, HID3, 256):
        if at + 256 < HID3:
            begin_chunk(at + 256)
        for lane in (at, at + 128):
            lanes = slice(lane, lane + 128)
            total = nothing
            for k in range(STEPS):
                rows = step_rows(k)
                active, slope = gelu_pair(hid3_ref[rows, lanes] + hid_bias3[:, lanes])
                u3_ref[rows, lanes] = active.astype(bf16)
                change = slope * dhid3_ref[rows, lanes]
                g3_ref[rows, lanes] = change.astype(bf16)
                total = total + fold(change)
            acc_hid_three[:, lanes] += total
        lanes = slice(at, at + 256)
        out = product(u3_ref[:, lanes], w4_ref[lanes])
        d_low = product_nt(g3_ref[:, lanes], w3_ref[:, lanes])
        result_ref[0] = out if at == 0 else result_ref[0] + out
        dx3_ref[...] = d_low if at == 0 else dx3_ref[...] + d_low
        keep(3, product_tn(h3_ref[...], g3_ref[:, lanes]), col=at)
        keep(4, product_tn(u3_ref[:, lanes], dy3_ref[...]), row=at)

    def finish3(k, carry):
        d_scale, d_shift, d_gain = carry
        rows = step_rows(k)
        valid = widen(inv3_ref[rows]) > 0.0
        mixed = mix3_ref[rows]
        out = jnp.where(valid, result_ref[0, rows] + out_bias3, 0.0)
        result_ref[0, rows] = mixed + scale4 * out
        d_scale = d_scale + fold(out * goal_ref[0, rows].astype(f32))
        d_low = dx3_ref[rows]
        normal = affine(mixed, *normal4)
        return (d_scale, d_shift + fold(d_low), d_gain + fold(d_low * normal))

    d_scale, d_shift, d_gain = sweep(finish3, (nothing3, nothing3, nothing3))
    acc_three[6] += d_scale
    acc_three[5] += d_shift
    acc_three[4] += d_gain
    mean_shift = by_image(d_shift * gain4) / count_three
    mean_gain = by_image(d_gain * gain4) / count_three
    back_gain4 = scaling4 * gain4
    back_mean4 = spread(-scaling4 * mean_shift, WIDE)
    back_normal4 = spread(scaling4 * mean_gain, WIDE)

    def unmix3(k, d_scale):
        rows = step_rows(k)
        share = widen(inv3_ref[rows])
        valid = share > 0.0
        normal = affine(mix3_ref[rows], *normal4)
        back = affine(dx3_ref[rows], back_gain4, back_mean4) - scaled(normal, back_normal4)
        d_mixed = jnp.where(valid, back + goal_ref[0, rows].astype(f32), 0.0)
        dx3_ref[rows] = d_mixed
        d_scale = d_scale + fold(pool3_ref[rows] * d_mixed)
        weighted = scale3 * d_mixed * share
        col3_ref[step_rows(k, 1)] = weighted + from_left(weighted) + from_right(weighted)
        return d_scale

    acc_three[3] += sweep(unmix3, nothing3)
    normal3 = (spread(scaling3, WIDE), spread(-mean3 * scaling3, WIDE))

    def unpool3(k, carry):
        d_shift, d_gain = carry
        rows = step_rows(k)
        valid = widen(inv3_ref[rows]) > 0.0
        d_normal = jnp.where(valid, row_windows3(k) - scale3 * dx3_ref[rows], 0.0)
        pool3_ref[rows] = d_normal
        normal = affine(e_ref[rows], *normal3)
        return (d_shift + fold(d_normal), d_gain + fold(d_normal * normal))

    d_shift, d_gain = sweep(unpool3, (nothing3, nothing3))
    acc_three[2] += d_shift
    acc_three[1] += d_gain
    mean_shift = by_image(d_shift * gain3) / count_three
    mean_gain = by_image(d_gain * gain3) / count_three
    back_gain3 = scaling3 * gain3
    back_mean3 = spread(-scaling3 * mean_shift, WIDE)
    back_normal3 = spread(scaling3 * mean_gain, WIDE)

    def unnorm3(k, d_bias):
        rows = step_rows(k)
        valid = widen(inv3_ref[rows]) > 0.0
        normal = affine(e_ref[rows], *normal3)
        back = affine(pool3_ref[rows], back_gain3, back_mean3) - scaled(normal, back_normal3)
        low = jnp.where(valid, dx3_ref[rows] + back, 0.0).astype(bf16)
        dpre_ref[rows] = low
        return d_bias + fold(low.astype(f32))

    acc_three[0] += sweep(unnorm3, nothing3)
    keep(2, product_tn(patch_ref[...], dpre_ref[...]))
    dpatch_ref[0:AREA] = product_nt(dpre_ref[...], we_ref[...])
    dpatch_ref[AREA : AREA + LINE] = jnp.zeros((LINE, 9 * C2), f32)

    def gather_back(k, carry):
        rows = step_rows(k)

        def tap(ky, kx, source):
            at = (3 * ky + kx) * C2
            value = dpatch_ref[source, at : at + C2]
            if ky != kx:
                at = (3 * kx + ky) * C2
                value = jnp.where(flipped, dpatch_ref[source, at : at + C2], value)
            return value

        sources = []
        for ky in range(3):
            source = step_rows(k, 1 if ky == 0 else 0)
            sources.append(
                (tap(ky, 1, source), tap(ky, 2, source) + from_right(tap(ky, 0, source)))
            )
        for pc in range(2):
            for pr, value in ((0, sources[1][pc]), (1, sources[2][pc] + sources[0][pc])):
                plane = pr * 2 + pc
                valid = inv_ref[plane, rows] > 0.0
                back_ref[plane, rows] = jnp.where(valid, rounded(value), 0.0)
        return carry

    sweep(gather_back, 0)

    normal2 = (spread(scaling2, C2), spread(-mean2 * scaling2, C2))

    def begin_back(plane):
        goal = scale2 * back_ref[plane]
        dy_ref[plane_rows(plane)] = goal.astype(bf16)
        hid_ref[plane % 2] = product_nt(goal.astype(bf16), w2_ref[...])
        return fold(goal)

    d_out_bias = begin_back(0)
    d_shift, d_gain = nothing, nothing
    sums = [nothing] * (HID2 // 128)
    new_gw1, new_gw2 = None, None
    for plane in range(4):
        if plane < 3:
            d_out_bias = d_out_bias + begin_back(plane + 1)
        for k in range(STEPS):
            rows = step_rows(k)
            part = slice(plane * AREA + k * STEP, plane * AREA + k * STEP + STEP)
            for n, at in enumerate(range(0, HID2, 128)):
                lanes = slice(at, at + 128)
                change = g_ref[part, lanes].astype(f32) * hid_ref[plane % 2, rows, lanes]
                g_ref[part, lanes] = change.astype(bf16)
                sums[n] = sums[n] + fold(change)
        flat = plane_rows(plane)
        d_low = product_nt(g_ref[flat], w1_ref[...])
        dx_ref[plane] = d_low
        d_shift = d_shift + fold(d_low)
        d_gain = d_gain + fold(d_low * affine(mix_ref[plane], *normal2))
        part_gw1 = product_tn(h_ref[flat], g_ref[flat])
        part_gw2 = product_tn(dy_ref[flat], u_ref[flat])
        new_gw1 = part_gw1 if plane == 0 else new_gw1 + part_gw1
        new_gw2 = part_gw2 if plane == 0 else new_gw2 + part_gw2
    new_gw2 = new_gw2.T
    for n, value in enumerate(sums):
        acc_hid_two[:, n * 128 : n * 128 + 128] += value
    acc_two[6] += d_out_bias
    acc_two[4] += d_shift
    acc_two[3] += d_gain
    mean_out[0, 0] = spread(by_image(d_shift * gain2) / count_two, 128)
    mean_out[0, 1] = spread(by_image(d_gain * gain2) / count_two, 128)
    keep(0, new_gw1)
    keep(1, new_gw2)
    d_scale = fold(w2_ref[...].astype(f32) * new_gw2) + out_bias * d_out_bias
    acc_two[5] += d_scale / scale2

    def finish():
        if pairs > 1:
            for which, ref in enumerate(grads):
                pack_part(which, ref[...])

        def filler(number, carry):
            put_block(number, jnp.zeros((HALF, 128), bf16))
            return carry

        lax.fori_loop(USED, slots, filler, 0)

        flat_ref[...] = jnp.zeros(flat_ref.shape, f32)

        def put(at, total, length):
            if at % 128:
                room = jnp.zeros((8, 128), f32)
                if total.shape[1] < length + BS:
                    total = jnp.concatenate([total, room], axis=1)
                total = pltpu.roll(total, BS, 1)
            whole = jnp.sum(total, axis=0, keepdims=True)
            done = -(at % 128)
            row = at // 128
            lane = 0
            while done < length:
                first = max(0, -done)
                last = min(128, length - done)
                flat_ref[row : row + 1, first:last] = whole[:, lane + first : lane + last]
                done += 128
                lane += 128
                row += 1

        at = 3 * C2
        for n in range(3, 6):
            put(at, acc_two[n], C2)
            at += C2
        put(at, acc_hid_two[...], HID2)
        at += HID2
        put(at, acc_two[6], C2)
        at += C2
        for n in range(7):
            put(at, acc_three[n], C3)
            at += C3
        put(at, acc_hid_three[...], HID3)
        at += HID3
        put(at, acc_three[7], C3)

    at_pair(pairs - 1, finish)


def run_main(places, place, buckets, state, goal, vec, weights, strip_count):
    pairs = goal.shape[0]
    slots = places[0].shape[0]
    half = slots // 2 + 1
    if pairs == 1:
        state = held_in(pltpu.VMEM, *state)
    weights = held_in(pltpu.VMEM, *weights)
    _, inv, _, mix, stat = state
    state_shapes = [STATE[1], STATE[3], STATE[4]]
    wide_f32 = pltpu.VMEM((AREA, WIDE), f32)
    wide_bf16 = pltpu.VMEM((AREA, WIDE), bf16)
    scratch = [
        pltpu.VMEM((4, AREA + LINE, C2), f32),
        pltpu.VMEM((2, AREA, HID2), f32),
        pltpu.VMEM((4 * AREA, HID2), bf16),
        pltpu.VMEM((4 * AREA, HID2), bf16),
        pltpu.VMEM((4 * AREA, C2), bf16),
        pltpu.VMEM((4 * AREA, C2), bf16),
        pltpu.VMEM((AREA, 9 * C2), bf16),
        pltpu.VMEM((AREA + LINE, 9 * C2), f32),
        pltpu.VMEM((AREA, 128), f32),
        wide_f32,
        pltpu.VMEM((AREA + 2 * LINE, WIDE), f32),
        wide_f32,
        wide_f32,
        wide_f32,
        pltpu.VMEM((AREA, HID3), f32),
        pltpu.VMEM((AREA, HID3), f32),
        pltpu.VMEM((AREA, HID3), bf16),
        pltpu.VMEM((AREA, HID3), bf16),
        wide_bf16,
        wide_bf16,
        wide_bf16,
        *[pltpu.VMEM(shape if pairs > 1 else (8, 128), f32) for shape in WEIGHTS],
        pltpu.VMEM((7, 8, C2), f32),
        pltpu.VMEM((8, HID2), f32),
        pltpu.VMEM((8, 8, WIDE), f32),
        pltpu.VMEM((8, HID3), f32),
    ]
    out_shapes = [(half, HALF, 128), (half, HALF, 128), (VEC_BLOCKS * HALF, 128)]
    make = pltpu.VMEM if pairs == 1 else jax.ShapeDtypeStruct
    return pl.pallas_call(
        functools.partial(main_kernel, pairs, strip_count, slots),
        grid=() if pairs == 1 else (pairs,),
        in_specs=[SMEM] * 4
        + pair_specs(pairs, state_shapes + [goal.shape[1:]], pl.Buffered(1))
        + whole_specs(pairs, [vec.shape])
        + [VMEM_BLOCK] * 5,
        out_specs=pair_specs(pairs, [(AREA, WIDE)] + BACK) + whole_specs(pairs, out_shapes),
        out_shape=pair_arrays(pairs, [(AREA, WIDE)] + BACK, [f32] * 4)
        + [make(shape, kind) for shape, kind in zip(out_shapes, (bf16, bf16, f32))],
        scratch_shapes=scratch,
        compiler_params=pltpu.CompilerParams(
            vmem_limit_bytes=(40 if pairs == 1 else 56) * 1024 * 1024,
        ),
        name="blocks",
    )(*places, place, buckets, inv, mix, stat, goal, vec, *weights)


def exit_kernel(
    pairs,
    strip_count,
    place_ref,
    bucket_ref,
    x_in,
    inv_in,
    pool_in,
    mix_in,
    stat_in,
    zed_in,
    dx_in,
    mean_in,
    flat_ref,
    vec_ref,
    payload_hbm,
    vector_ref,
    payload_ref,
    image_ref,
    col_ref,
    dx_ref,
    back_ref,
    acc_ref,
    sem,
):
    pair = pl.program_id(0) if pairs > 1 else 0
    x_ref, inv_ref, pool_ref, mix_ref, stat_ref, zed_ref, low_ref, mean_ref = (
        ref.at[0] for ref in (x_in, inv_in, pool_in, mix_in, stat_in, zed_in, dx_in, mean_in)
    )
    bucket_of = bucket_reader(place_ref, bucket_ref, strip_count)
    shape = Geometry(bucket_of, pair)
    count_two = shape.count_two
    gain1, bias1, scale1, gain2 = (vec_ref[n : n + 1] for n in range(4))
    mean1, scaling1, mean2, scaling2 = (stat_ref[n] for n in range(4))
    normal2 = (scaling2, -mean2 * scaling2)
    clear_edges(col_ref)
    nothing = jnp.zeros((8, C2), f32)
    back_gain2 = scaling2 * gain2
    back_mean2 = -scaling2 * mean_ref[0]
    back_normal2 = scaling2 * mean_ref[1]

    if pairs > 1:

        @pl.when(pair == 0)
        def _():
            acc_ref[...] = jnp.zeros(acc_ref.shape, f32)

    def add_up(n, total):
        acc_ref[n] = total if pairs == 1 else acc_ref[n] + total

    def unmix(k, d_scale):
        rows = step_rows(k)
        for pr in range(2):
            weighted = []
            for pc in range(2):
                plane = pr * 2 + pc
                share = inv_ref[plane, rows]
                normal = affine(mix_ref[plane, rows], *normal2)
                back = affine(low_ref[plane, rows], back_gain2, back_mean2)
                back = back - scaled(normal, back_normal2)
                d_mixed = jnp.where(share > 0.0, zed_ref[plane, rows] + back, 0.0)
                dx_ref[plane, rows] = d_mixed
                d_scale = d_scale + fold(pool_ref[plane, rows] * d_mixed)
                weighted.append(scale1 * d_mixed * share)
            put_col_windows(col_ref, pr, k, *weighted)
        return d_scale

    add_up(2, sweep(unmix, nothing))
    normal1 = (spread(scaling1, C2), spread(-mean1 * scaling1, C2))

    def unpool(k, carry):
        d_shift, d_gain = carry
        rows = step_rows(k)
        for pc in range(2):
            windows = row_windows(col_ref, pc, k)
            for pr in range(2):
                plane = pr * 2 + pc
                valid = inv_ref[plane, rows] > 0.0
                d_normal = windows[pr] - scale1 * dx_ref[plane, rows]
                d_normal = jnp.where(valid, d_normal, 0.0)
                back_ref[plane, rows] = d_normal
                normal = affine(x_ref[plane, rows], *normal1)
                d_shift = d_shift + fold(d_normal)
                d_gain = d_gain + fold(d_normal * normal)
        return (d_shift, d_gain)

    d_shift, d_gain = sweep(unpool, (nothing, nothing))
    add_up(1, d_shift)
    add_up(0, d_gain)
    mean_shift = by_image(d_shift * gain1) / count_two
    mean_gain = by_image(d_gain * gain1) / count_two
    back_gain1 = scaling1 * gain1
    back_mean1 = spread(-scaling1 * mean_shift, C2)
    back_normal1 = spread(scaling1 * mean_gain, C2)

    def unnorm(k, carry):
        rows = step_rows(k)
        for plane in range(4):
            normal = affine(x_ref[plane, rows], *normal1)
            back = affine(back_ref[plane, rows], back_gain1, back_mean1)
            back = back - scaled(normal, back_normal1)
            valid = inv_ref[plane, rows] > 0.0
            dx_ref[plane, rows] = jnp.where(valid, dx_ref[plane, rows] + back, 0.0)
        return carry

    sweep(unnorm, 0)

    def give_back(plane, here, spot, there):
        image_ref[spot, there] = dx_ref[plane, here]

    image_ref[...] = jnp.zeros(image_ref.shape, f32)
    each_image(bucket_of, pair, give_back)

    for spot in range(2 * STRIPS):
        target = strip_place(pair, spot, strip_count)
        for within in range(SR):
            rows = slice(within * CW, within * CW + CW)
            payload_ref[target, within] = image_ref[spot, rows].astype(bf16)

    def finish():
        copy = pltpu.make_async_copy(payload_ref, payload_hbm, sem)
        copy.start()
        vector_ref[...] = flat_ref[...]
        for n in range(3):
            vector_ref[n : n + 1] = jnp.sum(acc_ref[n], axis=0, keepdims=True)
        copy.wait()

    if pairs == 1:
        finish()
    else:
        pl.when(pair == pairs - 1)(finish)


def run_exit(place, buckets, state, back, flat, vec, strip_count):
    pairs = strip_count // 8
    payload = (strip_count, SR, CW, C2)
    make = pltpu.VMEM if pairs == 1 else jax.ShapeDtypeStruct
    plane_f32 = pltpu.VMEM((4, AREA, C2), f32)
    arrays = [*state, *back]
    if pairs == 1:
        arrays = held_in(pltpu.VMEM, *arrays)
    return pl.pallas_call(
        functools.partial(exit_kernel, pairs, strip_count),
        grid=() if pairs == 1 else (pairs,),
        in_specs=[SMEM] * 2
        + pair_specs(pairs, STATE + BACK, pl.Buffered(1))
        + whole_specs(pairs, [flat.shape, vec.shape]),
        out_specs=[HBM] + whole_specs(pairs, [flat.shape]),
        out_shape=[pltpu.HBM(payload, bf16), make(flat.shape, f32)],
        scratch_shapes=[
            pltpu.VMEM(payload, bf16),
            pltpu.VMEM((2 * STRIPS, STRIP_ROWS, C2), f32),
            pltpu.VMEM((4, AREA + 2 * LINE, C2), f32),
            plane_f32,
            plane_f32,
            pltpu.VMEM((3, 8, C2), f32),
            pltpu.SemaphoreType.DMA,
        ],
        compiler_params=roomy(8 if pairs == 1 else 40),
        name="exit",
    )(place, buckets, *arrays, flat, vec)


def dense_blocks(values):
    return jnp.concatenate([values[:, :HALF], values[:, HALF:]], axis=2).astype(bf16)


def pack_kernel(master_ref, dense_ref):
    dense_ref[...] = dense_blocks(master_ref[...])


def pack(master):
    owned = master.shape[0]
    return pl.pallas_call(
        pack_kernel,
        out_shape=jax.ShapeDtypeStruct((owned, HALF, 2 * BS), bf16),
        name="pack",
    )(master)


def pack_pieces_kernel(place_ref, master_hbm, pixel_hbm, *refs):
    out_refs, (wide_ref, master_ref, pixel_ref, sem) = refs[:-4], refs[-4:]
    owned = master_ref.shape[0]
    slots = pixel_ref.shape[2]
    copies = [pltpu.make_async_copy(pixel_hbm, pixel_ref, sem.at[0])]
    parts = [(0, owned // 2), (owned // 2, owned - owned // 2)]
    for n, part in enumerate(parts):
        copies.append(
            pltpu.make_async_copy(
                master_hbm.at[pl.ds(*part)], master_ref.at[pl.ds(*part)], sem.at[1 + n]
            )
        )
    for copy in copies:
        copy.start()
    copies[0].wait()

    def widen_row(row, carry):
        start = pl.multiple_of(row * CW * slots, 8)
        values = pixel_ref[row].astype(f32).reshape(CW * slots, C2)
        wide_ref[pl.ds(start, CW * slots)] = values
        return carry

    lax.fori_loop(0, SR, widen_row, 0)
    for k, ref in enumerate(out_refs):
        for other in range(2):
            slot = place_ref[0] ^ (2 * k + other)
            first = other * (ref.shape[0] - STRIP_ROWS)
            strip = wide_ref[pl.ds(slot, STRIP_ROWS, stride=slots)]
            ref[first : first + STRIP_ROWS] = strip.astype(bf16)
    for (first, count), copy in zip(parts, copies[1:]):
        copy.wait()
        dense = dense_blocks(master_ref[first : first + count]).reshape(count * HALF, 2 * BS)
        start = STRIP_ROWS + first * HALF
        for ref in out_refs[:3]:
            ref[start : start + count * HALF] = dense


def pack_pieces(place, master, pixels):
    slots = pixels.shape[2]
    rows = master.shape[0] * HALF
    shapes = [(rows + 2 * STRIP_ROWS, 2 * BS)] * 3 + [(2 * STRIP_ROWS, 2 * BS)]
    return pl.pallas_call(
        pack_pieces_kernel,
        in_specs=[SMEM] + [HBM] * 2,
        out_specs=[VMEM_BLOCK] * 4,
        out_shape=[pltpu.VMEM(shape, bf16) for shape in shapes],
        scratch_shapes=[
            pltpu.VMEM((STRIP_ROWS * slots, C2), f32),
            pltpu.VMEM(master.shape, f32),
            pltpu.VMEM(pixels.shape, bf16),
            pltpu.SemaphoreType.DMA((3,)),
        ],
        compiler_params=roomy(12),
        name="pack",
    )(place, *held_in(pltpu.HBM, master, pixels))


def fold_pair_kernel(near_ref, got_ref, own_ref, *part_refs):
    share = own_ref.shape[0]

    def one(n, carry):
        own_ref[n] = near_ref[n].astype(f32) + got_ref[n].astype(f32)
        for k, ref in enumerate(part_refs):
            here = (k + 1) * share + n
            ref[n] = near_ref[here] + got_ref[here]
        return carry

    lax.fori_loop(0, share, one, 0, unroll=4)


def fold_pair(near, got, groups):
    shape = ((near.shape[0] - 1) // groups,) + near.shape[1:]
    return pl.pallas_call(
        fold_pair_kernel,
        in_specs=[VMEM_BLOCK] * 2,
        out_specs=[VMEM_BLOCK] * groups,
        out_shape=[pltpu.VMEM(shape, f32)] + [pltpu.VMEM(shape, bf16)] * (groups - 1),
        compiler_params=roomy(4),
        name="fold_pair",
    )(*held_in(pltpu.VMEM, near, got))


def fold_tile_kernel(pieces, spot_ref, *refs):
    piece_refs, refs = refs[:pieces], refs[pieces:]
    vector_refs, refs = refs[:pieces], refs[pieces:]
    out_refs, sum_ref = refs[:-1], refs[-1]
    groups = len(out_refs)
    share = out_refs[0].shape[0]
    owned = piece_refs[0].shape[0]
    total = vector_refs[0][...].astype(f32)
    for ref in vector_refs[1:]:
        total = total + ref[...].astype(f32)
    for n in range(sum_ref.shape[0]):
        sum_ref[n] = jnp.zeros((HALF, 128), f32)
    for first in range(0, VEC_SENT, 16):
        at = first % HALF
        sum_ref[first // HALF, at : at + 16] = total[first : first + 16]

    def one(n, carry):
        for k, out_ref in enumerate(out_refs):
            number = lax.rem(spot_ref[0] + k, groups) * share + n
            block = jnp.minimum(number, owned - 1)
            total = piece_refs[0][block].astype(f32)
            for ref in piece_refs[1:]:
                total = total + ref[block].astype(f32)
            rest = sum_ref[jnp.maximum(number - owned, 0)]
            out_ref[n] = jnp.where(number < owned, total, rest).astype(out_ref.dtype)
        return carry

    lax.fori_loop(0, share, one, 0, unroll=share <= 16)


def fold_tile(spot, pieces, vectors, extra, groups):
    shape = ((pieces[0].shape[0] + extra) // groups,) + pieces[0].shape[1:]
    return pl.pallas_call(
        functools.partial(fold_tile_kernel, len(pieces)),
        in_specs=[SMEM] + [VMEM_BLOCK] * (len(pieces) + len(vectors)),
        out_specs=[VMEM_BLOCK] * groups,
        out_shape=[pltpu.VMEM(shape, f32)] + [pltpu.VMEM(shape, bf16)] * (groups - 1),
        scratch_shapes=[pltpu.VMEM((extra, HALF, 128), f32)],
        compiler_params=roomy(8),
        name="fold_tile",
    )(spot, *held_in(pltpu.VMEM, *pieces, *vectors))


def fold_batch_kernel(owned, vector_weight, spot_ref, *refs):
    part_refs, (total_ref, norm_ref) = refs[:-2], refs[-2:]
    share = total_ref.shape[0]
    square = jnp.zeros((8, 128), f32)
    for n in range(share):
        total = part_refs[0][n].astype(f32)
        for ref in part_refs[1:]:
            total = total + ref[n].astype(f32)
        total_ref[n] = total.astype(bf16)
        weight = jnp.where(spot_ref[0] * share + n < owned, 1.0, vector_weight)
        square = square + weight * fold(total * total)
    square = jnp.sum(jnp.sum(square, axis=1, keepdims=True), axis=0, keepdims=True)
    norm_ref[...] = jnp.broadcast_to(square[None], norm_ref.shape)


def fold_batch(spot, parts, owned, tile_count):
    count = tile_count * len(parts)
    return pl.pallas_call(
        functools.partial(fold_batch_kernel, owned, 1.0 / tile_count),
        in_specs=[SMEM] + [VMEM_BLOCK] * len(parts),
        out_specs=[VMEM_BLOCK] * 2,
        out_shape=[pltpu.VMEM(parts[0].shape, bf16), pltpu.VMEM((count, 1, 128), f32)],
        name="fold_batch",
    )(spot, *held_in(pltpu.VMEM, *parts))


def update_kernel(owned, groups, spot_ref, norm_ref, *refs):
    quarters, refs = refs[:groups], refs[groups:]
    stat_hbm, out_hbm, (vector_ref, clip_ref), refs = refs[:5], refs[5:10], refs[10:12], refs[12:]
    stat_refs, out_refs, (in_sem, out_sem) = refs[:5], refs[5:10], refs[10:]
    master_ref, left_stat_ref, right_stat_ref, left_root_ref, right_root_ref = stat_refs
    grad_ref, left_ref, right_ref, new_ref, copy_ref = out_refs
    share = quarters[0].shape[0]
    spans = spans_of(owned)

    def copies_of(sources, targets, sems):
        return [
            [
                pltpu.make_async_copy(
                    source.at[pl.ds(*span)], target.at[pl.ds(*span)], sems.at[5 * n + k]
                )
                for k, (source, target) in enumerate(zip(sources, targets))
            ]
            for n, span in enumerate(spans)
        ]

    copies_in = copies_of(stat_hbm, stat_refs, in_sem)
    copies_out = copies_of(out_refs, out_hbm, out_sem)
    for copies in copies_in:
        for copy in copies:
            copy.start()
    norm = jnp.sqrt(jnp.sum(norm_ref[...], axis=0))
    factor = jnp.minimum(1.0, clip_limit / norm)
    left_half = lax.broadcasted_iota(jnp.int32, (HALF, 128), 1) < BS

    def summed(number):
        source = number // share
        local = number - source * share
        turn = lax.rem(spot_ref[0] - source + groups, groups)
        value = quarters[0][local].astype(f32)
        for k in range(1, groups):
            value = jnp.where(turn == k, quarters[k][local].astype(f32), value)
        return value * factor

    def side_by_side(first, count):
        sides = []
        for n in range(first, first + count, 2):
            dense = summed(n)
            turned = pltpu.roll(dense, BS, 1)
            if n + 1 < first + count:
                second = summed(n + 1)
                top = jnp.where(left_half, dense, pltpu.roll(second, BS, 1))
                low = jnp.where(left_half, turned, second)
                side = jnp.concatenate([top, low], axis=0)
                grad_ref[n + 1] = pltpu.roll(side, BS, 1)[:, :BS]
            else:
                side = jnp.concatenate([dense, turned], axis=0)[:, :BS]
            grad_ref[n] = side[:, :BS]
            sides.append(side.astype(bf16))
        return jnp.concatenate(sides, axis=1)

    def diagonal_of(count):
        order = (count * BS, count * BS)
        return lax.broadcasted_iota(jnp.int32, order, 0) // BS == (
            lax.broadcasted_iota(jnp.int32, order, 1) // BS
        )

    clip_ref[...] = norm
    for n in range(vector_ref.shape[0]):
        vector_ref[n] = summed(owned + n)
    for (first, length), arriving, leaving in zip(spans, copies_in, copies_out):
        parts = [(n, min(4, first + length - n)) for n in range(first, first + length, 4)]
        wides = [side_by_side(*part) for part in parts]
        tall = [
            jnp.where(diagonal_of(count), jnp.concatenate([wide] * count, axis=0), 0.0)
            for (_, count), wide in zip(parts, wides)
        ]
        lefts = [product_nt(one, wide) for one, wide in zip(tall, wides)]
        rights = [product_tn(wide, wide) for wide in wides]
        for copy in arriving:
            copy.wait()
        stepped = []
        for (start, count), wide in zip(parts, wides):
            roots = left_root_ref[pl.ds(start, count)].reshape(count * BS, BS).astype(bf16)
            stepped.append(product(roots, wide))
        for (start, count), left, right in zip(parts, lefts, rights):
            here = pl.ds(start, count)
            left_ref[here] = 0.5 * left_stat_ref[here] + 0.5 * left.reshape(count, BS, BS)
            for n in range(count):
                at = n // 2 * 128
                block = right[n * BS : n * BS + BS, at : min(at + 128, count * BS)]
                if n % 2:
                    block = pltpu.roll(block, BS, 1)
                right_ref[start + n] = 0.5 * right_stat_ref[start + n] + 0.5 * block[:, :BS]
        for (start, count), value in zip(parts, stepped):
            here = pl.ds(start, count)
            value = jnp.where(diagonal_of(count), value, 0.0).astype(bf16)
            roots = right_root_ref[here].reshape(count * BS, BS).astype(bf16)
            value = product(value, roots).reshape(count, BS, BS)
            new = master_ref[here] - rate_matrix * value
            new_ref[here] = new
            copy_ref[here] = new.astype(bf16)
        for copy in leaving:
            copy.start()
    for leaving in copies_out:
        for copy in leaving:
            copy.wait()


def spans_of(owned):
    spans = []
    first = 0
    while first < owned:
        length = min(8 if first == 0 else 12, owned - first)
        spans.append((first, length))
        first += length
    return spans


def update(spot, norm, quarters, extra, *stats):
    shape = stats[0].shape
    groups = len(quarters)
    types = [f32] * 4 + [bf16]
    steps = len(spans_of(shape[0]))
    return pl.pallas_call(
        functools.partial(update_kernel, shape[0], groups),
        in_specs=[SMEM] + [VMEM_BLOCK] * (groups + 1) + [HBM] * 5,
        out_specs=[HBM] * 5 + [VMEM_BLOCK] * 2,
        out_shape=[pltpu.HBM(shape, kind) for kind in types]
        + [
            pltpu.VMEM((extra, HALF, 128), f32),
            pltpu.VMEM((1, 128), f32),
        ],
        scratch_shapes=[pltpu.VMEM(shape, f32)] * 5
        + [pltpu.VMEM(shape, kind) for kind in types]
        + [
            pltpu.SemaphoreType.DMA((5 * steps,)),
            pltpu.SemaphoreType.DMA((5 * steps,)),
        ],
        compiler_params=roomy(20),
        name="update",
    )(spot, *held_in(pltpu.VMEM, norm, *quarters), *held_in(pltpu.HBM, *stats))


def share_out(pieces, axis):
    return lax.all_to_all(pieces, axis, split_axis=0, concat_axis=0, tiled=True)


def swap(piece, distance):
    count = lax.axis_size("tile")
    return lax.ppermute(piece, "tile", [(i, i ^ distance) for i in range(count)])


def on_device(
    pixels,
    buckets,
    slot_owner_table,
    out_grad,
    master,
    left_stat,
    right_stat,
    left_root,
    right_root,
    vectors,
    moment,
):
    tile_count = lax.axis_size("tile")
    tile_place = lax.axis_index("tile")
    slot_count = pixels.shape[2]
    group_count = tile_count // STRIPS
    pairs = group_count // 2
    owned = master.shape[0]
    slots = owned * tile_count
    batch_count = lax.axis_size("batch")
    spot = lax.axis_index("batch").astype(jnp.int32).reshape(1)
    extra = extra_of(owned, batch_count)
    place = tile_place.astype(jnp.int32).reshape(1)
    paired = tile_count == 8
    numbers = jnp.arange(slots, dtype=jnp.int32)
    slot_of = jnp.sum(
        jnp.where(slot_owner_table[None, :] == numbers[:, None], numbers[None, :], 0), axis=1
    )
    if paired:
        owner = slot_of // owned
        apart = owner ^ tile_place
        apart = (apart & 1) * (tile_count // 2) + (apart >> 1)
        slot_of = slot_of + owned * (apart - owner)
    half = slots // 2
    near_place = jnp.where(slot_of < half, slot_of, half)
    far_place = jnp.where(slot_of < half, half, slot_of - half)
    vec = vectors.reshape(-1, 128)
    turned = lax.dynamic_index_in_dim(
        buckets.reshape(group_count, slot_count), tile_place, 1, keepdims=False
    ) >= 2
    flips = turned.reshape(-1, 1, 1, 1)
    goal = out_grad.reshape(2 * pairs, H3, W3, C3)
    goal = jnp.where(flips, goal.transpose(0, 2, 1, 3), goal)[:, :LINES]
    goal = goal.reshape(pairs, 2, LINES, W3, C3).transpose(0, 2, 3, 1, 4)
    goal = goal.reshape(pairs, LINES, 2 * W3, C3)
    goal = jnp.pad(goal, ((0, 0), (0, 0), (0, LINE - 2 * W3), (0, WIDE - C3)))
    goal = goal.reshape(pairs, AREA, WIDE)

    if paired:
        own, for_x, for_y, for_both = pack_pieces(
            place, master, pixels[0, 0].transpose(1, 2, 0, 3)
        )
        goal, vec, slot_of, near_place, far_place, for_both = lax.optimization_barrier(
            (goal, vec, slot_of, near_place, far_place, for_both)
        )
        from_x, from_y, strips_both = swap(for_x, 2), swap(for_y, 4), swap(for_both, 6)
        near_half = (owned + 1) // 2
        middle = STRIP_ROWS + near_half * HALF
        first_half = swap(from_x[STRIP_ROWS:middle], 4)
        second_half = swap(from_y[middle : STRIP_ROWS + owned * HALF], 2)
        mine = [own, from_x, from_y, strips_both, first_half, second_half]
        both = mine + [swap(piece, 1) for piece in mine]
        strips = both[:4] + both[6:10]
        pieces = [both[n] for n in (0, 1, 2, 4, 5, 6, 7, 8, 10, 11)]
        spans = [(STRIP_ROWS, owned)] * 3 + [(0, near_half), (0, owned - near_half)]
        spans = spans * 2
    else:
        pieces = [lax.all_gather(pack(master), "tile", axis=0, tiled=True).reshape(-1, 2 * BS)]
        spans = [(0, slots)]
        strips = share_out(pixels.reshape(tile_count, STRIP, C2), "tile")
        strips = [jnp.pad(strips, ((0, 0), (0, STRIP_ROWS - STRIP), (0, 0)))]

    weights = run_unpack(slot_of, pieces, spans)
    state = run_entry(place, buckets, strips, vec, tile_count)
    result, *back, near, far, flat = run_main(
        (near_place, far_place),
        place,
        buckets,
        state,
        goal,
        vec,
        weights,
        tile_count,
    )
    pixel_back, vector = run_exit(place, buckets, state, back, flat, vec, tile_count)
    if paired:
        own, *parts = fold_pair(near, swap(far, 1), tile_count // 2)
        pieces = [own] + [swap(part, 2 * k + 2) for k, part in enumerate(parts)]
        vector, _ = lax.optimization_barrier((vector, parts[0]))
        vector = (vector + swap(vector, 1))[:VEC_SENT].astype(bf16)
        vectors_in = [vector] + [swap(vector, 2 * k) for k in range(1, tile_count // 2)]
    else:
        outgoing = jnp.concatenate([near[:half], far[:half]], axis=0)
        pieces = list(share_out(outgoing.reshape(tile_count, owned, HALF, 128), "tile"))
        vectors_in = list(lax.all_gather(vector[:VEC_SENT], "tile"))
    result, pieces[1] = lax.optimization_barrier((result, pieces[1]))
    result = result.reshape(pairs, LINES, LINE, WIDE)[:, :, : 2 * W3, :C3]
    result = result.reshape(pairs, LINES, W3, 2, C3).transpose(0, 3, 1, 2, 4)
    result = result.reshape(2 * pairs, LINES, W3, C3)
    result = jnp.pad(result, ((0, 0), (0, H3 - LINES), (0, 0), (0, 0)))
    result = jnp.where(flips, result.transpose(0, 2, 1, 3), result)
    result = result.reshape(out_grad.shape)
    result = with_layout_constraint(result, Layout(major_to_minor=(0, 1, 2, 4, 5, 3, 6)))
    result, vectors_in[0] = lax.optimization_barrier((result, vectors_in[0]))
    own, *parts = fold_tile(spot, pieces, vectors_in, extra, batch_count)
    pixel_back, parts[0] = lax.optimization_barrier((pixel_back, parts[0]))
    returned = share_out(pixel_back, "tile")
    parts = [
        lax.ppermute(part, "batch", [(i, (i + k + 1) % batch_count) for i in range(batch_count)])
        for k, part in enumerate(parts)
    ]
    quarter, norm = fold_batch(spot, [own] + parts, owned, tile_count)
    returned, norm = lax.optimization_barrier((returned, norm))
    norm = share_out(norm, ("batch", "tile"))
    returned = returned.astype(f32).reshape(pixels.shape)
    returned = with_layout_constraint(returned, Layout(major_to_minor=(0, 1, 3, 4, 2, 5)))
    returned, norm = lax.optimization_barrier((returned, norm))
    quarters = [quarter] + [
        lax.ppermute(quarter, "batch", [(i, (i + k) % batch_count) for i in range(batch_count)])
        for k in range(1, batch_count)
    ]
    block_grad, left_new, right_new, master_new, weight_copy, whole_vector, clip = update(
        spot, norm, quarters, extra, master, left_stat, right_stat, left_root, right_root
    )
    clip_norm = clip[0, 0]
    share = vectors.shape[0] // tile_count
    whole_vector = whole_vector.reshape(-1)
    vec_grad = lax.dynamic_slice_in_dim(whole_vector, tile_place * share, share, 0)
    vec_moment = moment + vec_grad * vec_grad
    own_vectors = lax.dynamic_slice_in_dim(vectors, tile_place * share, share, 0)
    vec_new = own_vectors - rate_vector * vec_grad / (jnp.sqrt(vec_moment) + eps_adagrad)
    return (
        result,
        returned,
        clip_norm,
        block_grad,
        left_new,
        right_new,
        master_new,
        weight_copy,
        vec_grad,
        vec_moment,
        vec_new,
    )


def solution(mesh):
    placed = (
        P("batch", "tile", None, None, None, None),
        P("batch"),
        P(),
        P("batch", "tile", None, None, None, None, None),
        P("tile", None, None),
        P("tile", None, None),
        P("tile", None, None),
        P("tile", None, None),
        P("tile", None, None),
        P(),
        P("tile"),
    )
    return jax.shard_map(
        on_device,
        mesh=mesh,
        in_specs=placed,
        out_specs=(
            P("batch", "tile", None, None, None, None, None),
            P("batch", "tile", None, None, None, None),
            P(),
            P("tile", None, None),
            P("tile", None, None),
            P("tile", None, None),
            P("tile", None, None),
            P("tile", None, None),
            P("tile"),
            P("tile"),
            P("tile"),
        ),
        check_vma=False,
    )
```

```python
import functools

import jax
import jax.numpy as jnp
from jax import lax
from jax.experimental import pallas as pl
from jax.experimental.layout import Layout, with_layout_constraint
from jax.experimental.pallas import tpu as pltpu
from jax.sharding import PartitionSpec as P

C2 = 128
HID2 = 512
C3 = 320
HID3 = 1280
CH = 36
CW = 36
STRIPS = 4
BS = 64
SR = CH // STRIPS
H3 = CH // 2
W3 = CW // 2
LONG = 7 * CH // 9
LINES = LONG // 2
WIDE = 384
LINE = 40
AREA = LINES * LINE
STEP = 2 * LINE
STEPS = AREA // STEP
HALF = BS // 2
PART3 = HID3 // 2
STRIP = SR * CW
STRIP_ROWS = STRIP + -STRIP % 16

eps_norm = 1e-05
clip_limit = 1.0
rate_matrix = 0.3
rate_vector = 0.3
eps_adagrad = 1e-08
f32 = jnp.float32
bf16 = jnp.bfloat16

SHAPES = [(C2, HID2), (HID2, C2), (9 * C2, C3), (C3, HID3), (HID3, C3)]
USED = sum(rows // BS * (cols // BS) for rows, cols in SHAPES)
VEC_ROWS = (6 * C2 + HID2 + C2 + C3 + 6 * C3 + HID3 + C3) // 128


VEC_BLOCKS = -(-VEC_ROWS // HALF)


def extra_of(owned, groups):
    return VEC_BLOCKS + -(owned + VEC_BLOCKS) % groups


def product(left, right):
    return jnp.dot(left, right, preferred_element_type=f32)


def product_nt(left, right):
    return lax.dot_general(left, right, (((1,), (1,)), ((), ())), preferred_element_type=f32)


def product_tn(left, right):
    return lax.dot_general(left, right, (((0,), (0,)), ((), ())), preferred_element_type=f32)


def gelu_pair(values):
    bell = jnp.exp2(values * values * (-0.5 * 1.4426950408889634))
    step = pl.reciprocal(1.0 + (0.3275911 * 0.7071067811865476) * jnp.abs(values), approx=True)
    tail = step * (
        0.5 * 0.254829592
        + step
        * (
            0.5 * -0.284496736
            + step
            * (0.5 * 1.421413741 + step * (0.5 * -1.453152027 + step * (0.5 * 1.061405429)))
        )
    )
    tail = tail * bell
    share = jnp.where(values >= 0.0, 1.0 - tail, tail)
    return (values * share, share + values * (bell * 0.3989422804014327))


def fold(values):
    chans = values.shape[-1]
    return jnp.sum(values.reshape(-1, 8, chans), axis=0)


def by_image(total):
    total = total + pltpu.roll(total, 4, 0)
    total = total + pltpu.roll(total, 2, 0)
    return jnp.sum(total, axis=1, keepdims=True)


def line(pattern):
    return jnp.concatenate([pattern] * (LINE // 8), axis=0)


def spread(pattern, chans):
    return jnp.broadcast_to(pattern, (8, chans))


def affine(values, factor, shift):
    tiles = values.reshape(-1, 8, values.shape[-1])
    return (tiles * factor + shift).reshape(values.shape)


def scaled(values, factor):
    tiles = values.reshape(-1, 8, values.shape[-1])
    return (tiles * factor).reshape(values.shape)


def from_left(values):
    return pltpu.roll(values, 2, 0)


def from_right(values):
    return pltpu.roll(values, values.shape[0] - 2, 0)


def rounded(values):
    return values.astype(bf16).astype(f32)


def widen(values):
    return jnp.concatenate([values] * (WIDE // 128), axis=-1)


def norm_terms(total, square, count):
    mean = by_image(total) / count
    scaling = lax.rsqrt(by_image(square) / count - mean * mean + eps_norm)
    return (mean, scaling)


def sweep(visit, start):
    return lax.fori_loop(0, STEPS, visit, start, unroll=True)


def step_rows(k, lines=0):
    start = k * STEP + lines * LINE
    return pl.ds(start if isinstance(k, int) else pl.multiple_of(start, LINE), STEP)


def held_in(space, *arrays):
    return [pltpu.with_memory_space_constraint(array, space) for array in arrays]


VMEM_BLOCK = pl.BlockSpec(memory_space=pltpu.VMEM)
HBM = pl.BlockSpec(memory_space=pltpu.HBM)
SMEM = pl.BlockSpec(memory_space=pltpu.SMEM)


def roomy(mebibytes):
    return pltpu.CompilerParams(vmem_limit_bytes=mebibytes * 1024 * 1024)


def image_shape(bucket_of, pair, image):
    bucket = bucket_of(2 * pair + image)
    plain = jnp.where(bucket == 0, 5 * CH // 9, 7 * CH // 9)
    across = jnp.where(bucket == 0, CW, 7 * CW // 9)
    turned = (bucket >= 2).astype(jnp.int32)
    return (
        jnp.where(turned > 0, 5 * CW // 9, plain),
        jnp.where(turned > 0, CH, across),
        turned,
    )


def bucket_reader(place_ref, bucket_ref, strip_count):
    return lambda group: bucket_ref[group * strip_count + place_ref[0]]


class Geometry:
    def __init__(self, bucket_of, pair):
        parity = lax.broadcasted_iota(jnp.int32, (8, 128), 0) % 2
        even, odd = (image_shape(bucket_of, pair, image) for image in range(2))
        high, broad, turned = (jnp.where(parity == 0, a, b) for a, b in zip(even, odd))
        self.high = high
        self.count_two = (high * broad * C2).astype(f32)[:, :1]
        self.high3 = (high + 1) // 2
        broad3 = (broad + 1) // 2
        self.count_three = (self.high3 * broad3 * C3).astype(f32)[:, :1]
        place = lax.broadcasted_iota(jnp.int32, (LINE, 128), 0) // 2
        inside = lax.broadcasted_iota(jnp.int32, (LINE, 128), 0) < 2 * W3
        self.reach = []
        self.col_share = []
        for pc in range(2):
            column = 2 * place + pc
            self.reach.append(jnp.where(inside & (column < line(broad)), line(high), 0))
            edge = (column == 0) | (column == line(broad) - 1)
            self.col_share.append(jnp.where(edge, 0.5, 1.0 / 3.0))
        self.reach3 = jnp.where(inside & (place < line(broad3)), line(self.high3), 0)
        edge3 = (place == 0) | (place == line(broad3) - 1)
        self.col_share3 = jnp.where(edge3, 0.5, 1.0 / 3.0)
        self.flipped = jnp.concatenate([turned] * (STEP // 8), axis=0) > 0

    def share(self, plane, k):
        pr, pc = plane // 2, plane % 2
        return self.lines(4 * k + pr, 2, self.reach[pc], self.col_share[pc], self.high)

    def share3(self, k):
        return self.lines(2 * k, 1, self.reach3, self.col_share3, self.high3)

    def lines(self, row, stride, reach, col_share, height):
        parts = []
        for n in range(2):
            here = row + stride * n
            row_share = jnp.where((here == 0) | (here == height - 1), 0.5, 1.0 / 3.0)
            parts.append(jnp.where(here < reach, line(row_share) * col_share, 0.0))
        return jnp.concatenate(parts, axis=0)


def strip_place(pair, spot, strip_count):
    return lax.rem(pair * 8 + strip_count - 2 + spot, strip_count)


def each_image(bucket_of, pair, visit):
    for image in range(2):
        way = image_shape(bucket_of, pair, image)[2]

        @pl.when(way == 0)
        def _():
            def one(r, carry):
                for plane in range(4):
                    row = 2 * r + plane // 2
                    strip = row // SR
                    there = pl.ds((row - strip * SR) * CW + plane % 2, W3, stride=2)
                    here = pl.ds(r * LINE + image, W3, stride=2)
                    visit(plane, here, image * STRIPS + strip, there)
                return carry

            lax.fori_loop(0, LINES, one, 0)

        @pl.when(way == 1)
        def _():
            def one(r, carry):
                for plane in range(4):
                    for strip in range(STRIPS):
                        first = (plane % 2 + strip * SR) % 2
                        count = (SR - first + 1) // 2
                        done = (strip * SR + first) // 2
                        column = 2 * r + plane // 2
                        there = pl.ds(first * CW + column, count, stride=2 * CW)
                        here = pl.ds(r * LINE + image + 2 * done, count, stride=2)
                        visit(plane, here, image * STRIPS + strip, there)
                return carry

            lax.fori_loop(0, LINES, one, 0)


def row_windows(col_ref, pc, k):
    both = col_ref[pc, step_rows(k, 1)] + col_ref[2 + pc, step_rows(k, 1)]
    return (both + col_ref[2 + pc, step_rows(k)], both + col_ref[pc, step_rows(k, 2)])


def put_col_windows(col_ref, pr, k, even, odd):
    both = even + odd
    col_ref[pr * 2, step_rows(k, 1)] = both + from_left(odd)
    col_ref[pr * 2 + 1, step_rows(k, 1)] = both + from_right(even)


def clear_edges(col_ref):
    zero_line = jnp.zeros((LINE, C2), f32)
    for plane in range(4):
        col_ref[plane, 0:LINE] = zero_line
        col_ref[plane, AREA + LINE : AREA + 2 * LINE] = zero_line


def entry_kernel(pairs, strip_count, piece_count, place_ref, bucket_ref, vec_ref, *refs):
    piece_refs, refs = refs[:piece_count], refs[piece_count:]
    x_out, inv_out, pool_out, mix_out, stat_out, image_ref, col_ref = refs
    pair = pl.program_id(0) if pairs > 1 else 0
    x_ref, inv_ref, pool_ref, mix_ref = (ref.at[0] for ref in (x_out, inv_out, pool_out, mix_out))
    bucket_of = bucket_reader(place_ref, bucket_ref, strip_count)
    shape = Geometry(bucket_of, pair)
    gain1, bias1, scale1 = (vec_ref[n : n + 1] for n in range(3))
    clear_edges(col_ref)
    if piece_count > 1:
        half = piece_count // 2
        for n, ref in enumerate(piece_refs):
            source = place_ref[0] ^ (n // half + 2 * (n % half))
            spot = lax.rem(source + 2, 2 * STRIPS)
            first = 0 if n < half else ref.shape[0] - STRIP_ROWS
            image_ref[spot] = ref[first : first + STRIP_ROWS].astype(f32)
    else:
        for spot in range(2 * STRIPS):
            source = strip_place(pair, spot, strip_count)
            image_ref[spot] = piece_refs[0][source].astype(f32)

    def take_in(plane, here, spot, there):
        x_ref[plane, here] = image_ref[spot, there]

    each_image(bucket_of, pair, take_in)

    def arrange(k, carry):
        total, square = carry
        rows = step_rows(k)
        for plane in range(4):
            share = shape.share(plane, k)
            inv_ref[plane, rows] = share
            values = jnp.where(share > 0.0, x_ref[plane, rows], 0.0)
            x_ref[plane, rows] = values
            total = total + fold(values)
            square = square + fold(values * values)
        return (total, square)

    nothing = jnp.zeros((8, C2), f32)
    total, square = sweep(arrange, (nothing, nothing))
    mean1, scaling1 = norm_terms(total, square, shape.count_two)
    factor1 = scaling1 * gain1
    shift1 = bias1 - mean1 * scaling1 * gain1

    def window_cols(k, carry):
        rows = step_rows(k)
        for pr in range(2):
            masked = []
            for pc in range(2):
                plane = pr * 2 + pc
                normal = rounded(affine(x_ref[plane, rows], factor1, shift1))
                masked.append(jnp.where(inv_ref[plane, rows] > 0.0, normal, 0.0))
            put_col_windows(col_ref, pr, k, *masked)
        return carry

    sweep(window_cols, 0)

    def mix(k, carry):
        total, square = carry
        rows = step_rows(k)
        for pc in range(2):
            windows = row_windows(col_ref, pc, k)
            for pr in range(2):
                plane = pr * 2 + pc
                values = x_ref[plane, rows]
                share = inv_ref[plane, rows]
                pooled = windows[pr] * share - rounded(affine(values, factor1, shift1))
                pooled = jnp.where(share > 0.0, pooled, 0.0)
                mixed = values + scale1 * pooled
                pool_ref[plane, rows] = pooled
                mix_ref[plane, rows] = mixed
                total = total + fold(mixed)
                square = square + fold(mixed * mixed)
        return (total, square)

    total, square = sweep(mix, (nothing, nothing))
    mean2, scaling2 = norm_terms(total, square, shape.count_two)
    for n, value in enumerate((mean1, scaling1, mean2, scaling2)):
        stat_out[0, n] = spread(value, 128)


def pair_specs(pairs, shapes, mode=None):
    if pairs == 1:
        return [VMEM_BLOCK] * len(shapes)
    return [
        pl.BlockSpec(
            (1,) + shape, lambda t, rank=len(shape): (t,) + (0,) * rank, pipeline_mode=mode
        )
        for shape in shapes
    ]


def whole_specs(pairs, shapes):
    if pairs == 1:
        return [VMEM_BLOCK] * len(shapes)
    return [
        pl.BlockSpec(
            shape,
            lambda t, rank=len(shape): (0,) * rank,
            pipeline_mode=pl.Buffered(1),
        )
        for shape in shapes
    ]


def pair_arrays(pairs, shapes, kinds):
    make = pltpu.VMEM if pairs == 1 else jax.ShapeDtypeStruct
    return [make((pairs,) + shape, kind) for shape, kind in zip(shapes, kinds)]


STATE = [(4, AREA, C2)] * 4 + [(4, 8, 128)]
BACK = [(4, AREA, C2)] * 2 + [(2, 8, 128)]


def run_entry(place, buckets, pieces, vec, strip_count):
    pairs = strip_count // 8
    if pairs == 1:
        pieces = held_in(pltpu.VMEM, *pieces)
    return pl.pallas_call(
        functools.partial(entry_kernel, pairs, strip_count, len(pieces)),
        grid=() if pairs == 1 else (pairs,),
        in_specs=[SMEM] * 2 + whole_specs(pairs, [array.shape for array in (vec, *pieces)]),
        out_specs=pair_specs(pairs, STATE),
        out_shape=pair_arrays(pairs, STATE, [f32] * 5),
        scratch_shapes=[
            pltpu.VMEM((2 * STRIPS, STRIP_ROWS, C2), f32),
            pltpu.VMEM((4, AREA + 2 * LINE, C2), f32),
        ],
        compiler_params=roomy(6 if pairs == 1 else 40),
        name="entry",
    )(place, buckets, vec, *pieces)


WEIGHTS = [(C2, HID2), (HID2, C2), (9 * C2, WIDE), (WIDE, HID3), (HID3, WIDE)]


def unpack_kernel(spans, slot_ref, *refs):
    piece_refs, refs = refs[: len(spans)], refs[len(spans) :]
    weights, gathered_ref = refs[:-1], refs[-1]
    done = 0
    for ref, (first, count) in zip(piece_refs, spans):
        blocks = ref[first : first + count * HALF].reshape(count, HALF, 128)
        gathered_ref[done : done + count] = blocks
        done += count
    left_half = lax.broadcasted_iota(jnp.int32, (HALF, 128), 1) < BS
    offset = 0
    for (rows, cols), ref in zip(SHAPES, weights):
        wide = cols // BS
        for rb in range(rows // BS):
            for cb in range(0, wide, 2):
                number = offset + rb * wide + cb
                first = gathered_ref[slot_ref[number]]
                turned = pltpu.roll(first, BS, 1)
                if cb + 1 < wide:
                    second = gathered_ref[slot_ref[number + 1]]
                    top = jnp.where(left_half, first, pltpu.roll(second, BS, 1))
                    low = jnp.where(left_half, turned, second)
                else:
                    top = jnp.where(left_half, first, 0.0)
                    low = jnp.where(left_half, turned, 0.0)
                place = slice(cb * BS, cb * BS + 128)
                ref[rb * BS : rb * BS + HALF, place] = top
                ref[rb * BS + HALF : rb * BS + BS, place] = low
        offset += rows // BS * wide
    weights[3][C3:, :] = jnp.zeros((WIDE - C3, HID3), bf16)


def run_unpack(slot_of, pieces, spans):
    slots = slot_of.shape[0]
    return pl.pallas_call(
        functools.partial(unpack_kernel, spans),
        in_specs=[SMEM] + [VMEM_BLOCK] * len(pieces),
        out_specs=[VMEM_BLOCK] * 5,
        out_shape=[pltpu.VMEM(shape, bf16) for shape in WEIGHTS],
        scratch_shapes=[pltpu.VMEM((slots, HALF, 128), bf16)],
        compiler_params=roomy(6),
        name="unpack",
    )(slot_of, *held_in(pltpu.VMEM, *pieces))


def main_kernel(
    pairs,
    strip_count,
    slots,
    near_place,
    far_place,
    place_ref,
    bucket_ref,
    inv_in,
    mix_in,
    stat_in,
    goal_ref,
    vec_ref,
    w1_ref,
    w2_ref,
    we_ref,
    w3_ref,
    w4_ref,
    result_ref,
    zed_out,
    dx_out,
    mean_out,
    near_ref,
    far_ref,
    flat_ref,
    zed_ref,
    hid_ref,
    u_ref,
    g_ref,
    h_ref,
    dy_ref,
    patch_ref,
    dpatch_ref,
    inv3_ref,
    e_ref,
    col3_ref,
    pool3_ref,
    mix3_ref,
    dx3_ref,
    hid3_ref,
    dhid3_ref,
    u3_ref,
    g3_ref,
    h3_ref,
    dy3_ref,
    dpre_ref,
    gw1_ref,
    gw2_ref,
    gwe_ref,
    gw3_ref,
    gw4_ref,
    acc_two,
    acc_hid_two,
    acc_three,
    acc_hid_three,
):
    pair = pl.program_id(0) if pairs > 1 else 0
    grads = [gw1_ref, gw2_ref, gwe_ref, gw3_ref, gw4_ref]
    inv_ref, mix_ref, stat_ref = (ref.at[0] for ref in (inv_in, mix_in, stat_in))
    back_ref, dx_ref = zed_out.at[0], dx_out.at[0]
    left_half = lax.broadcasted_iota(jnp.int32, (HALF, 128), 1) < BS

    def at_pair(number, act):
        if pairs == 1:
            act()
        else:
            pl.when(pair == number)(act)

    def begin():
        acc_two[...] = jnp.zeros(acc_two.shape, f32)
        acc_hid_two[...] = jnp.zeros(acc_hid_two.shape, f32)
        acc_three[...] = jnp.zeros(acc_three.shape, f32)
        acc_hid_three[...] = jnp.zeros(acc_hid_three.shape, f32)

    at_pair(0, begin)
    shape = Geometry(bucket_reader(place_ref, bucket_ref, strip_count), pair)
    count_two, count_three, flipped = shape.count_two, shape.count_three, shape.flipped
    nothing = jnp.zeros((8, C2), f32)
    nothing3 = jnp.zeros((8, WIDE), f32)

    def vector_row(at, length):
        first, shift = at // 128, at % 128
        count = -(-(shift + length) // 128)
        row = jnp.concatenate([vec_ref[first + n : first + n + 1] for n in range(count)], axis=1)
        if shift:
            row = pltpu.roll(jnp.broadcast_to(row, (8, count * 128)), count * 128 - shift, 1)[:1]
        return row

    def wide_row(at):
        lane = lax.broadcasted_iota(jnp.int32, (1, WIDE), 1)
        return jnp.where(lane < C3, vector_row(at, C3)[:, :WIDE], 0.0)

    gain2, bias2, scale2 = (vec_ref[n : n + 1] for n in range(3, 6))
    hid_bias = vector_row(6 * C2, HID2)
    out_bias = vector_row(6 * C2 + HID2, C2)
    two = 7 * C2 + HID2
    embed_bias, gain3, bias3, scale3 = (wide_row(two + n * C3) for n in range(4))
    gain4, bias4, scale4 = (wide_row(two + n * C3) for n in range(4, 7))
    hid_bias3 = vector_row(two + 7 * C3, HID3)[:, :HID3]
    out_bias3 = wide_row(two + 7 * C3 + HID3)
    mean2, scaling2 = stat_ref[2], stat_ref[3]
    factor2 = scaling2 * gain2
    shift2 = bias2 - mean2 * scaling2 * gain2
    for plane in range(4):
        zed_ref[plane, 0:LINE] = jnp.zeros((LINE, C2), f32)
    col3_ref[0:LINE] = jnp.zeros((LINE, WIDE), f32)
    col3_ref[AREA + LINE : AREA + 2 * LINE] = jnp.zeros((LINE, WIDE), f32)

    def put_block(number, block):
        near_ref[near_place[number]] = block
        far_ref[far_place[number]] = block

    offsets = [0]
    for rows, cols in SHAPES:
        offsets.append(offsets[-1] + rows // BS * (cols // BS))

    def pack_part(which, values, row=0, col=0):
        rows, cols = SHAPES[which]
        wide = cols // BS
        values = values.astype(bf16)
        for rb in range(row // BS, min(rows, row + values.shape[0]) // BS):
            for cb in range(col // BS, min(cols, col + values.shape[1]) // BS, 2):
                number = offsets[which] + rb * wide + cb
                start = rb * BS - row
                at = slice(cb * BS - col, cb * BS - col + 128)
                top = values[start : start + HALF, at]
                low = values[start + HALF : start + BS, at]
                put_block(number, jnp.where(left_half, top, pltpu.roll(low, BS, 1)))
                if cb + 1 < wide:
                    put_block(number + 1, jnp.where(left_half, pltpu.roll(top, BS, 1), low))

    def plane_rows(plane):
        return slice(plane * AREA, plane * AREA + AREA)

    def begin_plane(plane):
        low = affine(mix_ref[plane], factor2, shift2).astype(bf16)
        h_ref[plane_rows(plane)] = low
        hid_ref[plane % 2] = product(low, w1_ref[...])

    begin_plane(0)
    for plane in range(4):
        if plane < 3:
            begin_plane(plane + 1)
        for k in range(STEPS):
            rows = step_rows(k)
            flat = slice(plane * AREA + k * STEP, plane * AREA + k * STEP + STEP)
            for at in range(0, HID2, 128):
                lanes = slice(at, at + 128)
                active, slope = gelu_pair(hid_ref[plane % 2, rows, lanes] + hid_bias[:, lanes])
                u_ref[flat, lanes] = active.astype(bf16)
                g_ref[flat, lanes] = slope.astype(bf16)
        out = product(u_ref[plane_rows(plane)], w2_ref[...]) + out_bias
        zed = jnp.where(inv_ref[plane] > 0.0, mix_ref[plane] + scale2 * out, 0.0)
        zed_ref[plane, LINE : LINE + AREA] = rounded(zed)

    def patches(k, carry):
        rows = step_rows(k)
        taps = []
        for ky in range(3):
            pr = (0 if ky == 1 else 1) * 2
            source = step_rows(k, 0 if ky == 0 else 1)
            even = zed_ref[pr, source]
            odd = zed_ref[pr + 1, source]
            taps.append((from_left(odd), even, odd))
        for ky in range(3):
            for kx in range(3):
                at = (3 * ky + kx) * C2
                tap = taps[ky][kx]
                if ky != kx:
                    tap = jnp.where(flipped, taps[kx][ky], tap)
                patch_ref[rows, at : at + C2] = tap.astype(bf16)
        return carry

    sweep(patches, 0)
    e_ref[...] = product(patch_ref[...], we_ref[...])

    def embed(k, carry):
        total, square = carry
        rows = step_rows(k)
        share = shape.share3(k)
        inv3_ref[rows] = share
        out = jnp.where(widen(share) > 0.0, e_ref[rows] + embed_bias, 0.0)
        e_ref[rows] = out
        return (total + fold(out), square + fold(out * out))

    total, square = sweep(embed, (nothing3, nothing3))
    mean3, scaling3 = norm_terms(total, square, count_three)
    factor3 = scaling3 * gain3
    shift3 = bias3 - mean3 * scaling3 * gain3

    def window_cols3(k, carry):
        rows = step_rows(k)
        normal = rounded(affine(e_ref[rows], factor3, shift3))
        masked = jnp.where(widen(inv3_ref[rows]) > 0.0, normal, 0.0)
        col3_ref[step_rows(k, 1)] = masked + from_left(masked) + from_right(masked)
        return carry

    sweep(window_cols3, 0)

    def row_windows3(k):
        return col3_ref[step_rows(k)] + col3_ref[step_rows(k, 1)] + col3_ref[step_rows(k, 2)]

    def mix3(k, carry):
        total, square = carry
        rows = step_rows(k)
        values = e_ref[rows]
        share = widen(inv3_ref[rows])
        pooled = row_windows3(k) * share - rounded(affine(values, factor3, shift3))
        pooled = jnp.where(share > 0.0, pooled, 0.0)
        mixed = values + scale3 * pooled
        pool3_ref[rows] = pooled
        mix3_ref[rows] = mixed
        return (total + fold(mixed), square + fold(mixed * mixed))

    total, square = sweep(mix3, (nothing3, nothing3))
    mean4, scaling4 = norm_terms(total, square, count_three)
    factor4 = scaling4 * gain4
    shift4 = bias4 - mean4 * scaling4 * gain4
    normal4 = (spread(scaling4, WIDE), spread(-mean4 * scaling4, WIDE))

    def prepare3(k, d_bias):
        rows = step_rows(k)
        h3_ref[rows] = affine(mix3_ref[rows], factor4, shift4).astype(bf16)
        goal = goal_ref[0, rows].astype(f32)
        goal = jnp.where(widen(inv3_ref[rows]) > 0.0, goal, 0.0)
        goal = scale4 * goal
        dy3_ref[rows] = goal.astype(bf16)
        return d_bias + fold(goal)

    acc_three[7] += sweep(prepare3, nothing3)

    def keep(which, value, row=0, col=0):
        if pairs == 1:
            pack_part(which, value, row, col)
        else:
            ref = grads[which]
            place = (slice(row, row + value.shape[0]), slice(col, col + value.shape[1]))

            @pl.when(pair == 0)
            def _():
                ref[place] = value

            @pl.when(pair > 0)
            def _():
                ref[place] += value

    def begin_chunk(at):
        lanes = slice(at, at + PART3)
        hid3_ref[:, lanes] = product(h3_ref[...], w3_ref[:, lanes])
        dhid3_ref[:, lanes] = product_nt(dy3_ref[...], w4_ref[lanes])

    begin_chunk(0)
    for at in range(0, HID3, PART3):
        if at + PART3 < HID3:
            begin_chunk(at + PART3)
        for lane in range(at, at + PART3, 128):
            lanes = slice(lane, lane + 128)
            total = nothing
            for k in range(STEPS):
                rows = step_rows(k)
                active, slope = gelu_pair(hid3_ref[rows, lanes] + hid_bias3[:, lanes])
                u3_ref[rows, lanes] = active.astype(bf16)
                change = slope * dhid3_ref[rows, lanes]
                g3_ref[rows, lanes] = change.astype(bf16)
                total = total + fold(change)
            acc_hid_three[:, lanes] += total
        lanes = slice(at, at + PART3)
        out = product(u3_ref[:, lanes], w4_ref[lanes])
        d_low = product_nt(g3_ref[:, lanes], w3_ref[:, lanes])
        result_ref[0] = out if at == 0 else result_ref[0] + out
        dx3_ref[...] = d_low if at == 0 else dx3_ref[...] + d_low
        keep(3, product_tn(h3_ref[...], g3_ref[:, lanes]), col=at)
        keep(4, product_tn(u3_ref[:, lanes], dy3_ref[...]), row=at)

    def finish3(k, carry):
        d_scale, d_shift, d_gain = carry
        rows = step_rows(k)
        valid = widen(inv3_ref[rows]) > 0.0
        mixed = mix3_ref[rows]
        out = jnp.where(valid, result_ref[0, rows] + out_bias3, 0.0)
        result_ref[0, rows] = mixed + scale4 * out
        d_scale = d_scale + fold(out * goal_ref[0, rows].astype(f32))
        d_low = dx3_ref[rows]
        normal = affine(mixed, *normal4)
        return (d_scale, d_shift + fold(d_low), d_gain + fold(d_low * normal))

    d_scale, d_shift, d_gain = sweep(finish3, (nothing3, nothing3, nothing3))
    acc_three[6] += d_scale
    acc_three[5] += d_shift
    acc_three[4] += d_gain
    mean_shift = by_image(d_shift * gain4) / count_three
    mean_gain = by_image(d_gain * gain4) / count_three
    back_gain4 = scaling4 * gain4
    back_mean4 = spread(-scaling4 * mean_shift, WIDE)
    back_normal4 = spread(scaling4 * mean_gain, WIDE)

    def unmix3(k, d_scale):
        rows = step_rows(k)
        share = widen(inv3_ref[rows])
        valid = share > 0.0
        normal = affine(mix3_ref[rows], *normal4)
        back = affine(dx3_ref[rows], back_gain4, back_mean4) - scaled(normal, back_normal4)
        d_mixed = jnp.where(valid, back + goal_ref[0, rows].astype(f32), 0.0)
        dx3_ref[rows] = d_mixed
        d_scale = d_scale + fold(pool3_ref[rows] * d_mixed)
        weighted = scale3 * d_mixed * share
        col3_ref[step_rows(k, 1)] = weighted + from_left(weighted) + from_right(weighted)
        return d_scale

    acc_three[3] += sweep(unmix3, nothing3)
    normal3 = (spread(scaling3, WIDE), spread(-mean3 * scaling3, WIDE))

    def unpool3(k, carry):
        d_shift, d_gain = carry
        rows = step_rows(k)
        valid = widen(inv3_ref[rows]) > 0.0
        d_normal = jnp.where(valid, row_windows3(k) - scale3 * dx3_ref[rows], 0.0)
        pool3_ref[rows] = d_normal
        normal = affine(e_ref[rows], *normal3)
        return (d_shift + fold(d_normal), d_gain + fold(d_normal * normal))

    d_shift, d_gain = sweep(unpool3, (nothing3, nothing3))
    acc_three[2] += d_shift
    acc_three[1] += d_gain
    mean_shift = by_image(d_shift * gain3) / count_three
    mean_gain = by_image(d_gain * gain3) / count_three
    back_gain3 = scaling3 * gain3
    back_mean3 = spread(-scaling3 * mean_shift, WIDE)
    back_normal3 = spread(scaling3 * mean_gain, WIDE)

    def unnorm3(k, d_bias):
        rows = step_rows(k)
        valid = widen(inv3_ref[rows]) > 0.0
        normal = affine(e_ref[rows], *normal3)
        back = affine(pool3_ref[rows], back_gain3, back_mean3) - scaled(normal, back_normal3)
        low = jnp.where(valid, dx3_ref[rows] + back, 0.0).astype(bf16)
        dpre_ref[rows] = low
        return d_bias + fold(low.astype(f32))

    acc_three[0] += sweep(unnorm3, nothing3)
    keep(2, product_tn(patch_ref[...], dpre_ref[...]))
    dpatch_ref[0:AREA] = product_nt(dpre_ref[...], we_ref[...])
    dpatch_ref[AREA : AREA + LINE] = jnp.zeros((LINE, 9 * C2), f32)

    def gather_back(k, carry):
        rows = step_rows(k)

        def tap(ky, kx, source):
            at = (3 * ky + kx) * C2
            value = dpatch_ref[source, at : at + C2]
            if ky != kx:
                at = (3 * kx + ky) * C2
                value = jnp.where(flipped, dpatch_ref[source, at : at + C2], value)
            return value

        sources = []
        for ky in range(3):
            source = step_rows(k, 1 if ky == 0 else 0)
            sources.append(
                (tap(ky, 1, source), tap(ky, 2, source) + from_right(tap(ky, 0, source)))
            )
        for pc in range(2):
            for pr, value in ((0, sources[1][pc]), (1, sources[2][pc] + sources[0][pc])):
                plane = pr * 2 + pc
                valid = inv_ref[plane, rows] > 0.0
                back_ref[plane, rows] = jnp.where(valid, rounded(value), 0.0)
        return carry

    sweep(gather_back, 0)

    normal2 = (spread(scaling2, C2), spread(-mean2 * scaling2, C2))

    def begin_back(plane):
        goal = scale2 * back_ref[plane]
        dy_ref[plane_rows(plane)] = goal.astype(bf16)
        hid_ref[plane % 2] = product_nt(goal.astype(bf16), w2_ref[...])
        return fold(goal)

    d_out_bias = begin_back(0)
    d_shift, d_gain = nothing, nothing
    sums = [nothing] * (HID2 // 128)
    new_gw1, new_gw2 = None, None
    for plane in range(4):
        if plane < 3:
            d_out_bias = d_out_bias + begin_back(plane + 1)
        for k in range(STEPS):
            rows = step_rows(k)
            part = slice(plane * AREA + k * STEP, plane * AREA + k * STEP + STEP)
            for n, at in enumerate(range(0, HID2, 128)):
                lanes = slice(at, at + 128)
                change = g_ref[part, lanes].astype(f32) * hid_ref[plane % 2, rows, lanes]
                g_ref[part, lanes] = change.astype(bf16)
                sums[n] = sums[n] + fold(change)
        flat = plane_rows(plane)
        d_low = product_nt(g_ref[flat], w1_ref[...])
        dx_ref[plane] = d_low
        d_shift = d_shift + fold(d_low)
        d_gain = d_gain + fold(d_low * affine(mix_ref[plane], *normal2))
        part_gw1 = product_tn(h_ref[flat], g_ref[flat])
        part_gw2 = product_tn(dy_ref[flat], u_ref[flat])
        new_gw1 = part_gw1 if plane == 0 else new_gw1 + part_gw1
        new_gw2 = part_gw2 if plane == 0 else new_gw2 + part_gw2
    new_gw2 = new_gw2.T
    for n, value in enumerate(sums):
        acc_hid_two[:, n * 128 : n * 128 + 128] += value
    acc_two[6] += d_out_bias
    acc_two[4] += d_shift
    acc_two[3] += d_gain
    mean_out[0, 0] = spread(by_image(d_shift * gain2) / count_two, 128)
    mean_out[0, 1] = spread(by_image(d_gain * gain2) / count_two, 128)
    keep(0, new_gw1)
    keep(1, new_gw2)
    d_scale = fold(w2_ref[...].astype(f32) * new_gw2) + out_bias * d_out_bias
    acc_two[5] += d_scale / scale2

    def finish():
        if pairs > 1:
            for which, ref in enumerate(grads):
                pack_part(which, ref[...])

        def filler(number, carry):
            put_block(number, jnp.zeros((HALF, 128), bf16))
            return carry

        lax.fori_loop(USED, slots, filler, 0)

        flat_ref[...] = jnp.zeros(flat_ref.shape, f32)

        def put(at, total, length):
            if at % 128:
                room = jnp.zeros((8, 128), f32)
                if total.shape[1] < length + BS:
                    total = jnp.concatenate([total, room], axis=1)
                total = pltpu.roll(total, BS, 1)
            whole = jnp.sum(total, axis=0, keepdims=True)
            done = -(at % 128)
            row = at // 128
            lane = 0
            while done < length:
                first = max(0, -done)
                last = min(128, length - done)
                flat_ref[row : row + 1, first:last] = whole[:, lane + first : lane + last]
                done += 128
                lane += 128
                row += 1

        at = 3 * C2
        for n in range(3, 6):
            put(at, acc_two[n], C2)
            at += C2
        put(at, acc_hid_two[...], HID2)
        at += HID2
        put(at, acc_two[6], C2)
        at += C2
        for n in range(7):
            put(at, acc_three[n], C3)
            at += C3
        put(at, acc_hid_three[...], HID3)
        at += HID3
        put(at, acc_three[7], C3)

    at_pair(pairs - 1, finish)


def run_main(places, place, buckets, state, goal, vec, weights, strip_count):
    pairs = goal.shape[0]
    slots = places[0].shape[0]
    half = slots // 2 + 1
    if pairs == 1:
        state = held_in(pltpu.VMEM, *state)
    weights = held_in(pltpu.VMEM, *weights)
    _, inv, _, mix, stat = state
    state_shapes = [STATE[1], STATE[3], STATE[4]]
    wide_f32 = pltpu.VMEM((AREA, WIDE), f32)
    wide_bf16 = pltpu.VMEM((AREA, WIDE), bf16)
    scratch = [
        pltpu.VMEM((4, AREA + LINE, C2), f32),
        pltpu.VMEM((2, AREA, HID2), f32),
        pltpu.VMEM((4 * AREA, HID2), bf16),
        pltpu.VMEM((4 * AREA, HID2), bf16),
        pltpu.VMEM((4 * AREA, C2), bf16),
        pltpu.VMEM((4 * AREA, C2), bf16),
        pltpu.VMEM((AREA, 9 * C2), bf16),
        pltpu.VMEM((AREA + LINE, 9 * C2), f32),
        pltpu.VMEM((AREA, 128), f32),
        wide_f32,
        pltpu.VMEM((AREA + 2 * LINE, WIDE), f32),
        wide_f32,
        wide_f32,
        wide_f32,
        pltpu.VMEM((AREA, HID3), f32),
        pltpu.VMEM((AREA, HID3), f32),
        pltpu.VMEM((AREA, HID3), bf16),
        pltpu.VMEM((AREA, HID3), bf16),
        wide_bf16,
        wide_bf16,
        wide_bf16,
        *[pltpu.VMEM(shape if pairs > 1 else (8, 128), f32) for shape in WEIGHTS],
        pltpu.VMEM((7, 8, C2), f32),
        pltpu.VMEM((8, HID2), f32),
        pltpu.VMEM((8, 8, WIDE), f32),
        pltpu.VMEM((8, HID3), f32),
    ]
    out_shapes = [(half, HALF, 128), (half, HALF, 128), (VEC_BLOCKS * HALF, 128)]
    make = pltpu.VMEM if pairs == 1 else jax.ShapeDtypeStruct
    return pl.pallas_call(
        functools.partial(main_kernel, pairs, strip_count, slots),
        grid=() if pairs == 1 else (pairs,),
        in_specs=[SMEM] * 4
        + pair_specs(pairs, state_shapes + [goal.shape[1:]], pl.Buffered(1))
        + whole_specs(pairs, [vec.shape])
        + [VMEM_BLOCK] * 5,
        out_specs=pair_specs(pairs, [(AREA, WIDE)] + BACK) + whole_specs(pairs, out_shapes),
        out_shape=pair_arrays(pairs, [(AREA, WIDE)] + BACK, [f32] * 4)
        + [make(shape, kind) for shape, kind in zip(out_shapes, (bf16, bf16, f32))],
        scratch_shapes=scratch,
        compiler_params=pltpu.CompilerParams(
            vmem_limit_bytes=(40 if pairs == 1 else 56) * 1024 * 1024,
        ),
        name="blocks",
    )(*places, place, buckets, inv, mix, stat, goal, vec, *weights)


def exit_kernel(
    pairs,
    strip_count,
    place_ref,
    bucket_ref,
    x_in,
    inv_in,
    pool_in,
    mix_in,
    stat_in,
    zed_in,
    dx_in,
    mean_in,
    flat_ref,
    vec_ref,
    payload_hbm,
    vector_ref,
    payload_ref,
    image_ref,
    col_ref,
    dx_ref,
    back_ref,
    acc_ref,
    sem,
):
    pair = pl.program_id(0) if pairs > 1 else 0
    x_ref, inv_ref, pool_ref, mix_ref, stat_ref, zed_ref, low_ref, mean_ref = (
        ref.at[0] for ref in (x_in, inv_in, pool_in, mix_in, stat_in, zed_in, dx_in, mean_in)
    )
    bucket_of = bucket_reader(place_ref, bucket_ref, strip_count)
    shape = Geometry(bucket_of, pair)
    count_two = shape.count_two
    gain1, bias1, scale1, gain2 = (vec_ref[n : n + 1] for n in range(4))
    mean1, scaling1, mean2, scaling2 = (stat_ref[n] for n in range(4))
    normal2 = (scaling2, -mean2 * scaling2)
    clear_edges(col_ref)
    nothing = jnp.zeros((8, C2), f32)
    back_gain2 = scaling2 * gain2
    back_mean2 = -scaling2 * mean_ref[0]
    back_normal2 = scaling2 * mean_ref[1]

    if pairs > 1:

        @pl.when(pair == 0)
        def _():
            acc_ref[...] = jnp.zeros(acc_ref.shape, f32)

    def add_up(n, total):
        acc_ref[n] = total if pairs == 1 else acc_ref[n] + total

    def unmix(k, d_scale):
        rows = step_rows(k)
        for pr in range(2):
            weighted = []
            for pc in range(2):
                plane = pr * 2 + pc
                share = inv_ref[plane, rows]
                normal = affine(mix_ref[plane, rows], *normal2)
                back = affine(low_ref[plane, rows], back_gain2, back_mean2)
                back = back - scaled(normal, back_normal2)
                d_mixed = jnp.where(share > 0.0, zed_ref[plane, rows] + back, 0.0)
                dx_ref[plane, rows] = d_mixed
                d_scale = d_scale + fold(pool_ref[plane, rows] * d_mixed)
                weighted.append(scale1 * d_mixed * share)
            put_col_windows(col_ref, pr, k, *weighted)
        return d_scale

    add_up(2, sweep(unmix, nothing))
    normal1 = (spread(scaling1, C2), spread(-mean1 * scaling1, C2))

    def unpool(k, carry):
        d_shift, d_gain = carry
        rows = step_rows(k)
        for pc in range(2):
            windows = row_windows(col_ref, pc, k)
            for pr in range(2):
                plane = pr * 2 + pc
                valid = inv_ref[plane, rows] > 0.0
                d_normal = windows[pr] - scale1 * dx_ref[plane, rows]
                d_normal = jnp.where(valid, d_normal, 0.0)
                back_ref[plane, rows] = d_normal
                normal = affine(x_ref[plane, rows], *normal1)
                d_shift = d_shift + fold(d_normal)
                d_gain = d_gain + fold(d_normal * normal)
        return (d_shift, d_gain)

    d_shift, d_gain = sweep(unpool, (nothing, nothing))
    add_up(1, d_shift)
    add_up(0, d_gain)
    mean_shift = by_image(d_shift * gain1) / count_two
    mean_gain = by_image(d_gain * gain1) / count_two
    back_gain1 = scaling1 * gain1
    back_mean1 = spread(-scaling1 * mean_shift, C2)
    back_normal1 = spread(scaling1 * mean_gain, C2)

    def unnorm(k, carry):
        rows = step_rows(k)
        for plane in range(4):
            normal = affine(x_ref[plane, rows], *normal1)
            back = affine(back_ref[plane, rows], back_gain1, back_mean1)
            back = back - scaled(normal, back_normal1)
            valid = inv_ref[plane, rows] > 0.0
            dx_ref[plane, rows] = jnp.where(valid, dx_ref[plane, rows] + back, 0.0)
        return carry

    sweep(unnorm, 0)

    def give_back(plane, here, spot, there):
        image_ref[spot, there] = dx_ref[plane, here]

    image_ref[...] = jnp.zeros(image_ref.shape, f32)
    each_image(bucket_of, pair, give_back)

    for spot in range(2 * STRIPS):
        target = strip_place(pair, spot, strip_count)
        for within in range(SR):
            rows = slice(within * CW, within * CW + CW)
            payload_ref[target, within] = image_ref[spot, rows].astype(bf16)

    def finish():
        copy = pltpu.make_async_copy(payload_ref, payload_hbm, sem)
        copy.start()
        vector_ref[...] = flat_ref[...]
        for n in range(3):
            vector_ref[n : n + 1] = jnp.sum(acc_ref[n], axis=0, keepdims=True)
        copy.wait()

    if pairs == 1:
        finish()
    else:
        pl.when(pair == pairs - 1)(finish)


def run_exit(place, buckets, state, back, flat, vec, strip_count):
    pairs = strip_count // 8
    payload = (strip_count, SR, CW, C2)
    make = pltpu.VMEM if pairs == 1 else jax.ShapeDtypeStruct
    plane_f32 = pltpu.VMEM((4, AREA, C2), f32)
    arrays = [*state, *back]
    if pairs == 1:
        arrays = held_in(pltpu.VMEM, *arrays)
    return pl.pallas_call(
        functools.partial(exit_kernel, pairs, strip_count),
        grid=() if pairs == 1 else (pairs,),
        in_specs=[SMEM] * 2
        + pair_specs(pairs, STATE + BACK, pl.Buffered(1))
        + whole_specs(pairs, [flat.shape, vec.shape]),
        out_specs=[HBM] + whole_specs(pairs, [flat.shape]),
        out_shape=[pltpu.HBM(payload, bf16), make(flat.shape, f32)],
        scratch_shapes=[
            pltpu.VMEM(payload, bf16),
            pltpu.VMEM((2 * STRIPS, STRIP_ROWS, C2), f32),
            pltpu.VMEM((4, AREA + 2 * LINE, C2), f32),
            plane_f32,
            plane_f32,
            pltpu.VMEM((3, 8, C2), f32),
            pltpu.SemaphoreType.DMA,
        ],
        compiler_params=roomy(8 if pairs == 1 else 40),
        name="exit",
    )(place, buckets, *arrays, flat, vec)


def dense_blocks(values):
    return jnp.concatenate([values[:, :HALF], values[:, HALF:]], axis=2).astype(bf16)


def pack_kernel(master_ref, dense_ref):
    dense_ref[...] = dense_blocks(master_ref[...])


def pack(master):
    owned = master.shape[0]
    return pl.pallas_call(
        pack_kernel,
        out_shape=jax.ShapeDtypeStruct((owned, HALF, 2 * BS), bf16),
        name="pack",
    )(master)


def pack_pieces_kernel(place_ref, master_hbm, pixel_hbm, *refs):
    out_refs, (wide_ref, master_ref, pixel_ref, sem) = refs[:-4], refs[-4:]
    owned = master_ref.shape[0]
    slots = pixel_ref.shape[2]
    copies = [pltpu.make_async_copy(pixel_hbm, pixel_ref, sem.at[0])]
    parts = [(0, owned // 2), (owned // 2, owned - owned // 2)]
    for n, part in enumerate(parts):
        copies.append(
            pltpu.make_async_copy(
                master_hbm.at[pl.ds(*part)], master_ref.at[pl.ds(*part)], sem.at[1 + n]
            )
        )
    for copy in copies:
        copy.start()
    copies[0].wait()

    def widen_row(row, carry):
        start = pl.multiple_of(row * CW * slots, 8)
        values = pixel_ref[row].astype(f32).reshape(CW * slots, C2)
        wide_ref[pl.ds(start, CW * slots)] = values
        return carry

    lax.fori_loop(0, SR, widen_row, 0)
    for k, ref in enumerate(out_refs):
        for other in range(2):
            slot = place_ref[0] ^ (2 * k + other)
            first = other * (ref.shape[0] - STRIP_ROWS)
            strip = wide_ref[pl.ds(slot, STRIP_ROWS, stride=slots)]
            ref[first : first + STRIP_ROWS] = strip.astype(bf16)
    for (first, count), copy in zip(parts, copies[1:]):
        copy.wait()
        dense = dense_blocks(master_ref[first : first + count]).reshape(count * HALF, 2 * BS)
        start = STRIP_ROWS + first * HALF
        for ref in out_refs[:3]:
            ref[start : start + count * HALF] = dense


def pack_pieces(place, master, pixels):
    slots = pixels.shape[2]
    rows = master.shape[0] * HALF
    shapes = [(rows + 2 * STRIP_ROWS, 2 * BS)] * 3 + [(2 * STRIP_ROWS, 2 * BS)]
    return pl.pallas_call(
        pack_pieces_kernel,
        in_specs=[SMEM] + [HBM] * 2,
        out_specs=[VMEM_BLOCK] * 4,
        out_shape=[pltpu.VMEM(shape, bf16) for shape in shapes],
        scratch_shapes=[
            pltpu.VMEM((STRIP_ROWS * slots, C2), f32),
            pltpu.VMEM(master.shape, f32),
            pltpu.VMEM(pixels.shape, bf16),
            pltpu.SemaphoreType.DMA((3,)),
        ],
        compiler_params=roomy(12),
        name="pack",
    )(place, *held_in(pltpu.HBM, master, pixels))


def fold_pair_kernel(near_ref, got_ref, own_ref, *part_refs):
    share = own_ref.shape[0]

    def one(n, carry):
        own_ref[n] = near_ref[n].astype(f32) + got_ref[n].astype(f32)
        for k, ref in enumerate(part_refs):
            here = (k + 1) * share + n
            ref[n] = near_ref[here] + got_ref[here]
        return carry

    lax.fori_loop(0, share, one, 0, unroll=4)


def fold_pair(near, got, groups):
    shape = ((near.shape[0] - 1) // groups,) + near.shape[1:]
    return pl.pallas_call(
        fold_pair_kernel,
        in_specs=[VMEM_BLOCK] * 2,
        out_specs=[VMEM_BLOCK] * groups,
        out_shape=[pltpu.VMEM(shape, f32)] + [pltpu.VMEM(shape, bf16)] * (groups - 1),
        compiler_params=roomy(4),
        name="fold_pair",
    )(*held_in(pltpu.VMEM, near, got))


def fold_tile_kernel(pieces, spot_ref, *refs):
    piece_refs, refs = refs[:pieces], refs[pieces:]
    vector_refs, refs = refs[:pieces], refs[pieces:]
    out_refs, sum_ref = refs[:-1], refs[-1]
    groups = len(out_refs)
    share = out_refs[0].shape[0]
    owned = piece_refs[0].shape[0]
    total = vector_refs[0][...]
    for ref in vector_refs[1:]:
        total = total + ref[...]
    for n in range(sum_ref.shape[0]):
        sum_ref[n] = jnp.zeros((HALF, 128), f32)
    for n in range(VEC_BLOCKS):
        sum_ref[n] = total[n * HALF : (n + 1) * HALF]

    def one(n, carry):
        for k, out_ref in enumerate(out_refs):
            number = lax.rem(spot_ref[0] + k, groups) * share + n
            block = jnp.minimum(number, owned - 1)
            total = piece_refs[0][block].astype(f32)
            for ref in piece_refs[1:]:
                total = total + ref[block].astype(f32)
            rest = sum_ref[jnp.maximum(number - owned, 0)]
            out_ref[n] = jnp.where(number < owned, total, rest).astype(out_ref.dtype)
        return carry

    lax.fori_loop(0, share, one, 0, unroll=share <= 16)


def fold_tile(spot, pieces, vectors, extra, groups):
    shape = ((pieces[0].shape[0] + extra) // groups,) + pieces[0].shape[1:]
    return pl.pallas_call(
        functools.partial(fold_tile_kernel, len(pieces)),
        in_specs=[SMEM] + [VMEM_BLOCK] * (len(pieces) + len(vectors)),
        out_specs=[VMEM_BLOCK] * groups,
        out_shape=[pltpu.VMEM(shape, f32)] + [pltpu.VMEM(shape, bf16)] * (groups - 1),
        scratch_shapes=[pltpu.VMEM((extra, HALF, 128), f32)],
        compiler_params=roomy(8),
        name="fold_tile",
    )(spot, *held_in(pltpu.VMEM, *pieces, *vectors))


def fold_batch_kernel(owned, vector_weight, spot_ref, *refs):
    part_refs, (total_ref, norm_ref) = refs[:-2], refs[-2:]
    share = total_ref.shape[0]
    square = jnp.zeros((8, 128), f32)
    for n in range(share):
        total = part_refs[0][n].astype(f32)
        for ref in part_refs[1:]:
            total = total + ref[n].astype(f32)
        total_ref[n] = total.astype(bf16)
        weight = jnp.where(spot_ref[0] * share + n < owned, 1.0, vector_weight)
        square = square + weight * fold(total * total)
    square = jnp.sum(jnp.sum(square, axis=1, keepdims=True), axis=0, keepdims=True)
    norm_ref[...] = jnp.broadcast_to(square[None], norm_ref.shape)


def fold_batch(spot, parts, owned, tile_count):
    count = tile_count * len(parts)
    return pl.pallas_call(
        functools.partial(fold_batch_kernel, owned, 1.0 / tile_count),
        in_specs=[SMEM] + [VMEM_BLOCK] * len(parts),
        out_specs=[VMEM_BLOCK] * 2,
        out_shape=[pltpu.VMEM(parts[0].shape, bf16), pltpu.VMEM((count, 1, 128), f32)],
        name="fold_batch",
    )(spot, *held_in(pltpu.VMEM, *parts))


def update_kernel(owned, groups, spot_ref, norm_ref, *refs):
    quarters, refs = refs[:groups], refs[groups:]
    stat_hbm, out_hbm, (vector_ref, clip_ref), refs = refs[:5], refs[5:10], refs[10:12], refs[12:]
    stat_refs, out_refs, (in_sem, out_sem) = refs[:5], refs[5:10], refs[10:]
    master_ref, left_stat_ref, right_stat_ref, left_root_ref, right_root_ref = stat_refs
    grad_ref, left_ref, right_ref, new_ref, copy_ref = out_refs
    share = quarters[0].shape[0]
    spans = spans_of(owned)

    def copies_of(sources, targets, sems):
        return [
            [
                pltpu.make_async_copy(
                    source.at[pl.ds(*span)], target.at[pl.ds(*span)], sems.at[5 * n + k]
                )
                for k, (source, target) in enumerate(zip(sources, targets))
            ]
            for n, span in enumerate(spans)
        ]

    copies_in = copies_of(stat_hbm, stat_refs, in_sem)
    copies_out = copies_of(out_refs, out_hbm, out_sem)
    for copies in copies_in:
        for copy in copies:
            copy.start()
    norm = jnp.sqrt(jnp.sum(norm_ref[...], axis=0))
    factor = jnp.minimum(1.0, clip_limit / norm)
    left_half = lax.broadcasted_iota(jnp.int32, (HALF, 128), 1) < BS

    def summed(number):
        source = number // share
        local = number - source * share
        turn = lax.rem(spot_ref[0] - source + groups, groups)
        value = quarters[0][local].astype(f32)
        for k in range(1, groups):
            value = jnp.where(turn == k, quarters[k][local].astype(f32), value)
        return value * factor

    def side_by_side(first, count):
        sides = []
        for n in range(first, first + count, 2):
            dense = summed(n)
            turned = pltpu.roll(dense, BS, 1)
            if n + 1 < first + count:
                second = summed(n + 1)
                top = jnp.where(left_half, dense, pltpu.roll(second, BS, 1))
                low = jnp.where(left_half, turned, second)
                side = jnp.concatenate([top, low], axis=0)
                grad_ref[n + 1] = pltpu.roll(side, BS, 1)[:, :BS]
            else:
                side = jnp.concatenate([dense, turned], axis=0)[:, :BS]
            grad_ref[n] = side[:, :BS]
            sides.append(side.astype(bf16))
        return jnp.concatenate(sides, axis=1)

    def diagonal_of(count):
        order = (count * BS, count * BS)
        return lax.broadcasted_iota(jnp.int32, order, 0) // BS == (
            lax.broadcasted_iota(jnp.int32, order, 1) // BS
        )

    clip_ref[...] = norm
    for n in range(vector_ref.shape[0]):
        vector_ref[n] = summed(owned + n)
    for (first, length), arriving, leaving in zip(spans, copies_in, copies_out):
        parts = [(n, min(4, first + length - n)) for n in range(first, first + length, 4)]
        wides = [side_by_side(*part) for part in parts]
        tall = [
            jnp.where(diagonal_of(count), jnp.concatenate([wide] * count, axis=0), 0.0)
            for (_, count), wide in zip(parts, wides)
        ]
        lefts = [product_nt(one, wide) for one, wide in zip(tall, wides)]
        rights = [product_tn(wide, wide) for wide in wides]
        for copy in arriving:
            copy.wait()
        stepped = []
        for (start, count), wide in zip(parts, wides):
            roots = left_root_ref[pl.ds(start, count)].reshape(count * BS, BS).astype(bf16)
            stepped.append(product(roots, wide))
        for (start, count), left, right in zip(parts, lefts, rights):
            here = pl.ds(start, count)
            left_ref[here] = 0.5 * left_stat_ref[here] + 0.5 * left.reshape(count, BS, BS)
            for n in range(count):
                at = n // 2 * 128
                block = right[n * BS : n * BS + BS, at : min(at + 128, count * BS)]
                if n % 2:
                    block = pltpu.roll(block, BS, 1)
                right_ref[start + n] = 0.5 * right_stat_ref[start + n] + 0.5 * block[:, :BS]
        for (start, count), value in zip(parts, stepped):
            here = pl.ds(start, count)
            value = jnp.where(diagonal_of(count), value, 0.0).astype(bf16)
            roots = right_root_ref[here].reshape(count * BS, BS).astype(bf16)
            value = product(value, roots).reshape(count, BS, BS)
            new = master_ref[here] - rate_matrix * value
            new_ref[here] = new
            copy_ref[here] = new.astype(bf16)
        for copy in leaving:
            copy.start()
    for leaving in copies_out:
        for copy in leaving:
            copy.wait()


def spans_of(owned):
    spans = []
    first = 0
    while first < owned:
        length = min(8 if first == 0 else 12, owned - first)
        spans.append((first, length))
        first += length
    return spans


def update(spot, norm, quarters, extra, *stats):
    shape = stats[0].shape
    groups = len(quarters)
    types = [f32] * 4 + [bf16]
    steps = len(spans_of(shape[0]))
    return pl.pallas_call(
        functools.partial(update_kernel, shape[0], groups),
        in_specs=[SMEM] + [VMEM_BLOCK] * (groups + 1) + [HBM] * 5,
        out_specs=[HBM] * 5 + [VMEM_BLOCK] * 2,
        out_shape=[pltpu.HBM(shape, kind) for kind in types]
        + [
            pltpu.VMEM((extra, HALF, 128), f32),
            pltpu.VMEM((1, 128), f32),
        ],
        scratch_shapes=[pltpu.VMEM(shape, f32)] * 5
        + [pltpu.VMEM(shape, kind) for kind in types]
        + [
            pltpu.SemaphoreType.DMA((5 * steps,)),
            pltpu.SemaphoreType.DMA((5 * steps,)),
        ],
        compiler_params=roomy(20),
        name="update",
    )(spot, *held_in(pltpu.VMEM, norm, *quarters), *held_in(pltpu.HBM, *stats))


def share_out(pieces, axis):
    return lax.all_to_all(pieces, axis, split_axis=0, concat_axis=0, tiled=True)


def swap(piece, distance):
    count = lax.axis_size("tile")
    return lax.ppermute(piece, "tile", [(i, i ^ distance) for i in range(count)])


def on_device(
    pixels,
    buckets,
    slot_owner_table,
    out_grad,
    master,
    left_stat,
    right_stat,
    left_root,
    right_root,
    vectors,
    moment,
):
    tile_count = lax.axis_size("tile")
    tile_place = lax.axis_index("tile")
    slot_count = pixels.shape[2]
    group_count = tile_count // STRIPS
    pairs = group_count // 2
    owned = master.shape[0]
    slots = owned * tile_count
    batch_count = lax.axis_size("batch")
    spot = lax.axis_index("batch").astype(jnp.int32).reshape(1)
    extra = extra_of(owned, batch_count)
    place = tile_place.astype(jnp.int32).reshape(1)
    paired = tile_count == 8
    numbers = jnp.arange(slots, dtype=jnp.int32)
    slot_of = jnp.sum(
        jnp.where(slot_owner_table[None, :] == numbers[:, None], numbers[None, :], 0), axis=1
    )
    if paired:
        owner = slot_of // owned
        apart = owner ^ tile_place
        apart = (apart & 1) * (tile_count // 2) + (apart >> 1)
        slot_of = slot_of + owned * (apart - owner)
    half = slots // 2
    near_place = jnp.where(slot_of < half, slot_of, half)
    far_place = jnp.where(slot_of < half, half, slot_of - half)
    vec = vectors.reshape(-1, 128)
    turned = lax.dynamic_index_in_dim(
        buckets.reshape(group_count, slot_count), tile_place, 1, keepdims=False
    ) >= 2
    flips = turned.reshape(-1, 1, 1, 1)
    goal = out_grad.reshape(2 * pairs, H3, W3, C3)
    goal = jnp.where(flips, goal.transpose(0, 2, 1, 3), goal)[:, :LINES]
    goal = goal.reshape(pairs, 2, LINES, W3, C3).transpose(0, 2, 3, 1, 4)
    goal = goal.reshape(pairs, LINES, 2 * W3, C3)
    goal = jnp.pad(goal, ((0, 0), (0, 0), (0, LINE - 2 * W3), (0, WIDE - C3)))
    goal = goal.reshape(pairs, AREA, WIDE)

    if paired:
        own, for_x, for_y, for_both = pack_pieces(
            place, master, pixels[0, 0].transpose(1, 2, 0, 3)
        )
        goal, vec, slot_of, near_place, far_place, for_both = lax.optimization_barrier(
            (goal, vec, slot_of, near_place, far_place, for_both)
        )
        from_x, from_y, strips_both = swap(for_x, 2), swap(for_y, 4), swap(for_both, 6)
        near_half = (owned + 1) // 2
        middle = STRIP_ROWS + near_half * HALF
        first_half = swap(from_x[STRIP_ROWS:middle], 4)
        second_half = swap(from_y[middle : STRIP_ROWS + owned * HALF], 2)
        mine = [own, from_x, from_y, strips_both, first_half, second_half]
        both = mine + [swap(piece, 1) for piece in mine]
        strips = both[:4] + both[6:10]
        pieces = [both[n] for n in (0, 1, 2, 4, 5, 6, 7, 8, 10, 11)]
        spans = [(STRIP_ROWS, owned)] * 3 + [(0, near_half), (0, owned - near_half)]
        spans = spans * 2
    else:
        pieces = [lax.all_gather(pack(master), "tile", axis=0, tiled=True).reshape(-1, 2 * BS)]
        spans = [(0, slots)]
        strips = share_out(pixels.reshape(tile_count, STRIP, C2), "tile")
        strips = [jnp.pad(strips, ((0, 0), (0, STRIP_ROWS - STRIP), (0, 0)))]

    weights = run_unpack(slot_of, pieces, spans)
    state = run_entry(place, buckets, strips, vec, tile_count)
    result, *back, near, far, flat = run_main(
        (near_place, far_place),
        place,
        buckets,
        state,
        goal,
        vec,
        weights,
        tile_count,
    )
    pixel_back, vector = run_exit(place, buckets, state, back, flat, vec, tile_count)
    if paired:
        own, *parts = fold_pair(near, swap(far, 1), tile_count // 2)
        pieces = [own] + [swap(part, 2 * k + 2) for k, part in enumerate(parts)]
        vector, _ = lax.optimization_barrier((vector, parts[0]))
        vector = vector + swap(vector, 1)
        vectors_in = [vector] + [swap(vector, 2 * k) for k in range(1, tile_count // 2)]
    else:
        outgoing = jnp.concatenate([near[:half], far[:half]], axis=0)
        pieces = list(share_out(outgoing.reshape(tile_count, owned, HALF, 128), "tile"))
        vectors_in = list(lax.all_gather(vector, "tile"))
    result, pieces[1] = lax.optimization_barrier((result, pieces[1]))
    result = result.reshape(pairs, LINES, LINE, WIDE)[:, :, : 2 * W3, :C3]
    result = result.reshape(pairs, LINES, W3, 2, C3).transpose(0, 3, 1, 2, 4)
    result = result.reshape(2 * pairs, LINES, W3, C3)
    result = jnp.pad(result, ((0, 0), (0, H3 - LINES), (0, 0), (0, 0)))
    result = jnp.where(flips, result.transpose(0, 2, 1, 3), result)
    result = result.reshape(out_grad.shape)
    result = with_layout_constraint(result, Layout(major_to_minor=(0, 1, 2, 4, 5, 3, 6)))
    result, vectors_in[0] = lax.optimization_barrier((result, vectors_in[0]))
    own, *parts = fold_tile(spot, pieces, vectors_in, extra, batch_count)
    pixel_back, parts[0] = lax.optimization_barrier((pixel_back, parts[0]))
    returned = share_out(pixel_back, "tile")
    parts = [
        lax.ppermute(part, "batch", [(i, (i + k + 1) % batch_count) for i in range(batch_count)])
        for k, part in enumerate(parts)
    ]
    quarter, norm = fold_batch(spot, [own] + parts, owned, tile_count)
    returned, norm = lax.optimization_barrier((returned, norm))
    norm = share_out(norm, ("batch", "tile"))
    returned = returned.astype(f32).reshape(pixels.shape)
    returned = with_layout_constraint(returned, Layout(major_to_minor=(0, 1, 3, 4, 2, 5)))
    returned, norm = lax.optimization_barrier((returned, norm))
    quarters = [quarter] + [
        lax.ppermute(quarter, "batch", [(i, (i + k) % batch_count) for i in range(batch_count)])
        for k in range(1, batch_count)
    ]
    block_grad, left_new, right_new, master_new, weight_copy, whole_vector, clip = update(
        spot, norm, quarters, extra, master, left_stat, right_stat, left_root, right_root
    )
    clip_norm = clip[0, 0]
    share = vectors.shape[0] // tile_count
    whole_vector = whole_vector.reshape(-1)
    vec_grad = lax.dynamic_slice_in_dim(whole_vector, tile_place * share, share, 0)
    vec_moment = moment + vec_grad * vec_grad
    own_vectors = lax.dynamic_slice_in_dim(vectors, tile_place * share, share, 0)
    vec_new = own_vectors - rate_vector * vec_grad / (jnp.sqrt(vec_moment) + eps_adagrad)
    return (
        result,
        returned,
        clip_norm,
        block_grad,
        left_new,
        right_new,
        master_new,
        weight_copy,
        vec_grad,
        vec_moment,
        vec_new,
    )


def solution(mesh):
    placed = (
        P("batch", "tile", None, None, None, None),
        P("batch"),
        P(),
        P("batch", "tile", None, None, None, None, None),
        P("tile", None, None),
        P("tile", None, None),
        P("tile", None, None),
        P("tile", None, None),
        P("tile", None, None),
        P(),
        P("tile"),
    )
    return jax.shard_map(
        on_device,
        mesh=mesh,
        in_specs=placed,
        out_specs=(
            P("batch", "tile", None, None, None, None, None),
            P("batch", "tile", None, None, None, None),
            P(),
            P("tile", None, None),
            P("tile", None, None),
            P("tile", None, None),
            P("tile", None, None),
            P("tile", None, None),
            P("tile"),
            P("tile"),
            P("tile"),
        ),
        check_vma=False,
    )
```

```python
import functools

import jax
import jax.numpy as jnp
from jax import lax
from jax.experimental import pallas as pl
from jax.experimental.layout import Layout, with_layout_constraint
from jax.experimental.pallas import tpu as pltpu
from jax.sharding import PartitionSpec as P

C2 = 128
HID2 = 512
C3 = 320
HID3 = 1280
CH = 36
CW = 36
STRIPS = 4
BS = 64
SR = CH // STRIPS
H3 = CH // 2
W3 = CW // 2
LONG = 7 * CH // 9
LINES = LONG // 2
WIDE = 384
LINE = 40
AREA = LINES * LINE
STEP = 2 * LINE
STEPS = AREA // STEP
HALF = BS // 2
STRIP = SR * CW
STRIP_ROWS = STRIP + -STRIP % 16

eps_norm = 1e-05
clip_limit = 1.0
rate_matrix = 0.3
rate_vector = 0.3
eps_adagrad = 1e-08
f32 = jnp.float32
bf16 = jnp.bfloat16

SHAPES = [(C2, HID2), (HID2, C2), (9 * C2, C3), (C3, HID3), (HID3, C3)]
USED = sum(rows // BS * (cols // BS) for rows, cols in SHAPES)
VEC_ROWS = (6 * C2 + HID2 + C2 + C3 + 6 * C3 + HID3 + C3) // 128


VEC_BLOCKS = -(-VEC_ROWS // HALF)


def extra_of(owned, groups):
    return VEC_BLOCKS + -(owned + VEC_BLOCKS) % groups


def product(left, right):
    return jnp.dot(left, right, preferred_element_type=f32)


def product_nt(left, right):
    return lax.dot_general(left, right, (((1,), (1,)), ((), ())), preferred_element_type=f32)


def product_tn(left, right):
    return lax.dot_general(left, right, (((0,), (0,)), ((), ())), preferred_element_type=f32)


def gelu_pair(values):
    bell = jnp.exp2(values * values * (-0.5 * 1.4426950408889634))
    step = pl.reciprocal(1.0 + (0.3275911 * 0.7071067811865476) * jnp.abs(values), approx=True)
    tail = step * (
        0.5 * 0.254829592
        + step
        * (
            0.5 * -0.284496736
            + step
            * (0.5 * 1.421413741 + step * (0.5 * -1.453152027 + step * (0.5 * 1.061405429)))
        )
    )
    tail = tail * bell
    share = jnp.where(values >= 0.0, 1.0 - tail, tail)
    return (values * share, share + values * (bell * 0.3989422804014327))


def fold(values):
    chans = values.shape[-1]
    return jnp.sum(values.reshape(-1, 8, chans), axis=0)


def by_image(total):
    total = total + pltpu.roll(total, 4, 0)
    total = total + pltpu.roll(total, 2, 0)
    return jnp.sum(total, axis=1, keepdims=True)


def line(pattern):
    return jnp.concatenate([pattern] * (LINE // 8), axis=0)


def spread(pattern, chans):
    return jnp.broadcast_to(pattern, (8, chans))


def affine(values, factor, shift):
    tiles = values.reshape(-1, 8, values.shape[-1])
    return (tiles * factor + shift).reshape(values.shape)


def scaled(values, factor):
    tiles = values.reshape(-1, 8, values.shape[-1])
    return (tiles * factor).reshape(values.shape)


def from_left(values):
    return pltpu.roll(values, 2, 0)


def from_right(values):
    return pltpu.roll(values, values.shape[0] - 2, 0)


def rounded(values):
    return values.astype(bf16).astype(f32)


def widen(values):
    return jnp.concatenate([values] * (WIDE // 128), axis=-1)


def norm_terms(total, square, count):
    mean = by_image(total) / count
    scaling = lax.rsqrt(by_image(square) / count - mean * mean + eps_norm)
    return (mean, scaling)


def sweep(visit, start):
    return lax.fori_loop(0, STEPS, visit, start, unroll=True)


def step_rows(k, lines=0):
    start = k * STEP + lines * LINE
    return pl.ds(start if isinstance(k, int) else pl.multiple_of(start, LINE), STEP)


def held_in(space, *arrays):
    return [pltpu.with_memory_space_constraint(array, space) for array in arrays]


VMEM_BLOCK = pl.BlockSpec(memory_space=pltpu.VMEM)
HBM = pl.BlockSpec(memory_space=pltpu.HBM)
SMEM = pl.BlockSpec(memory_space=pltpu.SMEM)


def roomy(mebibytes):
    return pltpu.CompilerParams(vmem_limit_bytes=mebibytes * 1024 * 1024)


def image_shape(bucket_of, pair, image):
    bucket = bucket_of(2 * pair + image)
    plain = jnp.where(bucket == 0, 5 * CH // 9, 7 * CH // 9)
    across = jnp.where(bucket == 0, CW, 7 * CW // 9)
    turned = (bucket >= 2).astype(jnp.int32)
    return (
        jnp.where(turned > 0, 5 * CW // 9, plain),
        jnp.where(turned > 0, CH, across),
        turned,
    )


def bucket_reader(place_ref, bucket_ref, strip_count):
    return lambda group: bucket_ref[group * strip_count + place_ref[0]]


class Geometry:
    def __init__(self, bucket_of, pair):
        parity = lax.broadcasted_iota(jnp.int32, (8, 128), 0) % 2
        even, odd = (image_shape(bucket_of, pair, image) for image in range(2))
        high, broad, turned = (jnp.where(parity == 0, a, b) for a, b in zip(even, odd))
        self.high = high
        self.count_two = (high * broad * C2).astype(f32)[:, :1]
        self.high3 = (high + 1) // 2
        broad3 = (broad + 1) // 2
        self.count_three = (self.high3 * broad3 * C3).astype(f32)[:, :1]
        place = lax.broadcasted_iota(jnp.int32, (LINE, 128), 0) // 2
        inside = lax.broadcasted_iota(jnp.int32, (LINE, 128), 0) < 2 * W3
        self.reach = []
        self.col_share = []
        for pc in range(2):
            column = 2 * place + pc
            self.reach.append(jnp.where(inside & (column < line(broad)), line(high), 0))
            edge = (column == 0) | (column == line(broad) - 1)
            self.col_share.append(jnp.where(edge, 0.5, 1.0 / 3.0))
        self.reach3 = jnp.where(inside & (place < line(broad3)), line(self.high3), 0)
        edge3 = (place == 0) | (place == line(broad3) - 1)
        self.col_share3 = jnp.where(edge3, 0.5, 1.0 / 3.0)
        self.flipped = jnp.concatenate([turned] * (STEP // 8), axis=0) > 0

    def share(self, plane, k):
        pr, pc = plane // 2, plane % 2
        return self.lines(4 * k + pr, 2, self.reach[pc], self.col_share[pc], self.high)

    def share3(self, k):
        return self.lines(2 * k, 1, self.reach3, self.col_share3, self.high3)

    def lines(self, row, stride, reach, col_share, height):
        parts = []
        for n in range(2):
            here = row + stride * n
            row_share = jnp.where((here == 0) | (here == height - 1), 0.5, 1.0 / 3.0)
            parts.append(jnp.where(here < reach, line(row_share) * col_share, 0.0))
        return jnp.concatenate(parts, axis=0)


def strip_place(pair, spot, strip_count):
    return lax.rem(pair * 8 + strip_count - 2 + spot, strip_count)


def each_image(bucket_of, pair, visit):
    for image in range(2):
        way = image_shape(bucket_of, pair, image)[2]

        @pl.when(way == 0)
        def _():
            def one(r, carry):
                for plane in range(4):
                    row = 2 * r + plane // 2
                    strip = row // SR
                    there = pl.ds((row - strip * SR) * CW + plane % 2, W3, stride=2)
                    here = pl.ds(r * LINE + image, W3, stride=2)
                    visit(plane, here, image * STRIPS + strip, there)
                return carry

            lax.fori_loop(0, LINES, one, 0)

        @pl.when(way == 1)
        def _():
            def one(r, carry):
                for plane in range(4):
                    for strip in range(STRIPS):
                        first = (plane % 2 + strip * SR) % 2
                        count = (SR - first + 1) // 2
                        done = (strip * SR + first) // 2
                        column = 2 * r + plane // 2
                        there = pl.ds(first * CW + column, count, stride=2 * CW)
                        here = pl.ds(r * LINE + image + 2 * done, count, stride=2)
                        visit(plane, here, image * STRIPS + strip, there)
                return carry

            lax.fori_loop(0, LINES, one, 0)


def row_windows(col_ref, pc, k):
    both = col_ref[pc, step_rows(k, 1)] + col_ref[2 + pc, step_rows(k, 1)]
    return (both + col_ref[2 + pc, step_rows(k)], both + col_ref[pc, step_rows(k, 2)])


def put_col_windows(col_ref, pr, k, even, odd):
    both = even + odd
    col_ref[pr * 2, step_rows(k, 1)] = both + from_left(odd)
    col_ref[pr * 2 + 1, step_rows(k, 1)] = both + from_right(even)


def clear_edges(col_ref):
    zero_line = jnp.zeros((LINE, C2), f32)
    for plane in range(4):
        col_ref[plane, 0:LINE] = zero_line
        col_ref[plane, AREA + LINE : AREA + 2 * LINE] = zero_line


def entry_kernel(pairs, strip_count, piece_count, place_ref, bucket_ref, vec_ref, *refs):
    piece_refs, refs = refs[:piece_count], refs[piece_count:]
    x_out, inv_out, pool_out, mix_out, stat_out, image_ref, col_ref = refs
    pair = pl.program_id(0) if pairs > 1 else 0
    x_ref, inv_ref, pool_ref, mix_ref = (ref.at[0] for ref in (x_out, inv_out, pool_out, mix_out))
    bucket_of = bucket_reader(place_ref, bucket_ref, strip_count)
    shape = Geometry(bucket_of, pair)
    gain1, bias1, scale1 = (vec_ref[n : n + 1] for n in range(3))
    clear_edges(col_ref)
    if piece_count > 1:
        half = piece_count // 2
        for n, ref in enumerate(piece_refs):
            source = place_ref[0] ^ (n // half + 2 * (n % half))
            spot = lax.rem(source + 2, 2 * STRIPS)
            first = 0 if n < half else ref.shape[0] - STRIP_ROWS
            image_ref[spot] = ref[first : first + STRIP_ROWS].astype(f32)
    else:
        for spot in range(2 * STRIPS):
            source = strip_place(pair, spot, strip_count)
            image_ref[spot] = piece_refs[0][source].astype(f32)

    def take_in(plane, here, spot, there):
        x_ref[plane, here] = image_ref[spot, there]

    each_image(bucket_of, pair, take_in)

    def arrange(k, carry):
        total, square = carry
        rows = step_rows(k)
        for plane in range(4):
            share = shape.share(plane, k)
            inv_ref[plane, rows] = share
            values = jnp.where(share > 0.0, x_ref[plane, rows], 0.0)
            x_ref[plane, rows] = values
            total = total + fold(values)
            square = square + fold(values * values)
        return (total, square)

    nothing = jnp.zeros((8, C2), f32)
    total, square = sweep(arrange, (nothing, nothing))
    mean1, scaling1 = norm_terms(total, square, shape.count_two)
    factor1 = scaling1 * gain1
    shift1 = bias1 - mean1 * scaling1 * gain1

    def window_cols(k, carry):
        rows = step_rows(k)
        for pr in range(2):
            masked = []
            for pc in range(2):
                plane = pr * 2 + pc
                normal = rounded(affine(x_ref[plane, rows], factor1, shift1))
                masked.append(jnp.where(inv_ref[plane, rows] > 0.0, normal, 0.0))
            put_col_windows(col_ref, pr, k, *masked)
        return carry

    sweep(window_cols, 0)

    def mix(k, carry):
        total, square = carry
        rows = step_rows(k)
        for pc in range(2):
            windows = row_windows(col_ref, pc, k)
            for pr in range(2):
                plane = pr * 2 + pc
                values = x_ref[plane, rows]
                share = inv_ref[plane, rows]
                pooled = windows[pr] * share - rounded(affine(values, factor1, shift1))
                pooled = jnp.where(share > 0.0, pooled, 0.0)
                mixed = values + scale1 * pooled
                pool_ref[plane, rows] = pooled
                mix_ref[plane, rows] = mixed
                total = total + fold(mixed)
                square = square + fold(mixed * mixed)
        return (total, square)

    total, square = sweep(mix, (nothing, nothing))
    mean2, scaling2 = norm_terms(total, square, shape.count_two)
    for n, value in enumerate((mean1, scaling1, mean2, scaling2)):
        stat_out[0, n] = spread(value, 128)


def pair_specs(pairs, shapes, mode=None):
    if pairs == 1:
        return [VMEM_BLOCK] * len(shapes)
    return [
        pl.BlockSpec(
            (1,) + shape, lambda t, rank=len(shape): (t,) + (0,) * rank, pipeline_mode=mode
        )
        for shape in shapes
    ]


def whole_specs(pairs, shapes):
    if pairs == 1:
        return [VMEM_BLOCK] * len(shapes)
    return [
        pl.BlockSpec(
            shape,
            lambda t, rank=len(shape): (0,) * rank,
            pipeline_mode=pl.Buffered(1),
        )
        for shape in shapes
    ]


def pair_arrays(pairs, shapes, kinds):
    make = pltpu.VMEM if pairs == 1 else jax.ShapeDtypeStruct
    return [make((pairs,) + shape, kind) for shape, kind in zip(shapes, kinds)]


STATE = [(4, AREA, C2)] * 4 + [(4, 8, 128)]
BACK = [(4, AREA, C2)] * 2 + [(2, 8, 128)]


def run_entry(place, buckets, pieces, vec, strip_count):
    pairs = strip_count // 8
    if pairs == 1:
        pieces = held_in(pltpu.VMEM, *pieces)
    return pl.pallas_call(
        functools.partial(entry_kernel, pairs, strip_count, len(pieces)),
        grid=() if pairs == 1 else (pairs,),
        in_specs=[SMEM] * 2 + whole_specs(pairs, [array.shape for array in (vec, *pieces)]),
        out_specs=pair_specs(pairs, STATE),
        out_shape=pair_arrays(pairs, STATE, [f32] * 5),
        scratch_shapes=[
            pltpu.VMEM((2 * STRIPS, STRIP_ROWS, C2), f32),
            pltpu.VMEM((4, AREA + 2 * LINE, C2), f32),
        ],
        compiler_params=roomy(6 if pairs == 1 else 40),
        name="entry",
    )(place, buckets, vec, *pieces)


WEIGHTS = [(C2, HID2), (HID2, C2), (9 * C2, WIDE), (WIDE, HID3), (HID3, WIDE)]


def unpack_kernel(spans, slot_ref, *refs):
    piece_refs, refs = refs[: len(spans)], refs[len(spans) :]
    weights, gathered_ref = refs[:-1], refs[-1]
    done = 0
    for ref, (first, count) in zip(piece_refs, spans):
        blocks = ref[first : first + count * HALF].reshape(count, HALF, 128)
        gathered_ref[done : done + count] = blocks
        done += count
    left_half = lax.broadcasted_iota(jnp.int32, (HALF, 128), 1) < BS
    offset = 0
    for (rows, cols), ref in zip(SHAPES, weights):
        wide = cols // BS
        for rb in range(rows // BS):
            for cb in range(0, wide, 2):
                number = offset + rb * wide + cb
                first = gathered_ref[slot_ref[number]]
                turned = pltpu.roll(first, BS, 1)
                if cb + 1 < wide:
                    second = gathered_ref[slot_ref[number + 1]]
                    top = jnp.where(left_half, first, pltpu.roll(second, BS, 1))
                    low = jnp.where(left_half, turned, second)
                else:
                    top = jnp.where(left_half, first, 0.0)
                    low = jnp.where(left_half, turned, 0.0)
                place = slice(cb * BS, cb * BS + 128)
                ref[rb * BS : rb * BS + HALF, place] = top
                ref[rb * BS + HALF : rb * BS + BS, place] = low
        offset += rows // BS * wide
    weights[3][C3:, :] = jnp.zeros((WIDE - C3, HID3), bf16)


def run_unpack(slot_of, pieces, spans):
    slots = slot_of.shape[0]
    return pl.pallas_call(
        functools.partial(unpack_kernel, spans),
        in_specs=[SMEM] + [VMEM_BLOCK] * len(pieces),
        out_specs=[VMEM_BLOCK] * 5,
        out_shape=[pltpu.VMEM(shape, bf16) for shape in WEIGHTS],
        scratch_shapes=[pltpu.VMEM((slots, HALF, 128), bf16)],
        compiler_params=roomy(6),
        name="unpack",
    )(slot_of, *held_in(pltpu.VMEM, *pieces))


def main_kernel(
    pairs,
    strip_count,
    slots,
    near_place,
    far_place,
    place_ref,
    bucket_ref,
    inv_in,
    mix_in,
    stat_in,
    goal_ref,
    vec_ref,
    w1_ref,
    w2_ref,
    we_ref,
    w3_ref,
    w4_ref,
    result_ref,
    zed_out,
    dx_out,
    mean_out,
    near_ref,
    far_ref,
    flat_ref,
    zed_ref,
    hid_ref,
    u_ref,
    g_ref,
    h_ref,
    dy_ref,
    patch_ref,
    dpatch_ref,
    inv3_ref,
    e_ref,
    col3_ref,
    pool3_ref,
    mix3_ref,
    dx3_ref,
    hid3_ref,
    dhid3_ref,
    u3_ref,
    g3_ref,
    h3_ref,
    dy3_ref,
    dpre_ref,
    gw1_ref,
    gw2_ref,
    gwe_ref,
    gw3_ref,
    gw4_ref,
    acc_two,
    acc_hid_two,
    acc_three,
    acc_hid_three,
):
    pair = pl.program_id(0) if pairs > 1 else 0
    grads = [gw1_ref, gw2_ref, gwe_ref, gw3_ref, gw4_ref]
    inv_ref, mix_ref, stat_ref = (ref.at[0] for ref in (inv_in, mix_in, stat_in))
    back_ref, dx_ref = zed_out.at[0], dx_out.at[0]
    left_half = lax.broadcasted_iota(jnp.int32, (HALF, 128), 1) < BS

    def at_pair(number, act):
        if pairs == 1:
            act()
        else:
            pl.when(pair == number)(act)

    def begin():
        acc_two[...] = jnp.zeros(acc_two.shape, f32)
        acc_hid_two[...] = jnp.zeros(acc_hid_two.shape, f32)
        acc_three[...] = jnp.zeros(acc_three.shape, f32)
        acc_hid_three[...] = jnp.zeros(acc_hid_three.shape, f32)

    at_pair(0, begin)
    shape = Geometry(bucket_reader(place_ref, bucket_ref, strip_count), pair)
    count_two, count_three, flipped = shape.count_two, shape.count_three, shape.flipped
    nothing = jnp.zeros((8, C2), f32)
    nothing3 = jnp.zeros((8, WIDE), f32)

    def vector_row(at, length):
        first, shift = at // 128, at % 128
        count = -(-(shift + length) // 128)
        row = jnp.concatenate([vec_ref[first + n : first + n + 1] for n in range(count)], axis=1)
        if shift:
            row = pltpu.roll(jnp.broadcast_to(row, (8, count * 128)), count * 128 - shift, 1)[:1]
        return row

    def wide_row(at):
        lane = lax.broadcasted_iota(jnp.int32, (1, WIDE), 1)
        return jnp.where(lane < C3, vector_row(at, C3)[:, :WIDE], 0.0)

    gain2, bias2, scale2 = (vec_ref[n : n + 1] for n in range(3, 6))
    hid_bias = vector_row(6 * C2, HID2)
    out_bias = vector_row(6 * C2 + HID2, C2)
    two = 7 * C2 + HID2
    embed_bias, gain3, bias3, scale3 = (wide_row(two + n * C3) for n in range(4))
    gain4, bias4, scale4 = (wide_row(two + n * C3) for n in range(4, 7))
    hid_bias3 = vector_row(two + 7 * C3, HID3)[:, :HID3]
    out_bias3 = wide_row(two + 7 * C3 + HID3)
    mean2, scaling2 = stat_ref[2], stat_ref[3]
    factor2 = scaling2 * gain2
    shift2 = bias2 - mean2 * scaling2 * gain2
    for plane in range(4):
        zed_ref[plane, 0:LINE] = jnp.zeros((LINE, C2), f32)
    col3_ref[0:LINE] = jnp.zeros((LINE, WIDE), f32)
    col3_ref[AREA + LINE : AREA + 2 * LINE] = jnp.zeros((LINE, WIDE), f32)

    def put_block(number, block):
        near_ref[near_place[number]] = block
        far_ref[far_place[number]] = block

    offsets = [0]
    for rows, cols in SHAPES:
        offsets.append(offsets[-1] + rows // BS * (cols // BS))

    def pack_part(which, values, row=0, col=0):
        rows, cols = SHAPES[which]
        wide = cols // BS
        values = values.astype(bf16)
        for rb in range(row // BS, min(rows, row + values.shape[0]) // BS):
            for cb in range(col // BS, min(cols, col + values.shape[1]) // BS, 2):
                number = offsets[which] + rb * wide + cb
                start = rb * BS - row
                at = slice(cb * BS - col, cb * BS - col + 128)
                top = values[start : start + HALF, at]
                low = values[start + HALF : start + BS, at]
                put_block(number, jnp.where(left_half, top, pltpu.roll(low, BS, 1)))
                if cb + 1 < wide:
                    put_block(number + 1, jnp.where(left_half, pltpu.roll(top, BS, 1), low))

    def plane_rows(plane):
        return slice(plane * AREA, plane * AREA + AREA)

    def begin_plane(plane):
        low = affine(mix_ref[plane], factor2, shift2).astype(bf16)
        h_ref[plane_rows(plane)] = low
        hid_ref[plane % 2] = product(low, w1_ref[...])

    begin_plane(0)
    for plane in range(4):
        if plane < 3:
            begin_plane(plane + 1)
        for k in range(STEPS):
            rows = step_rows(k)
            flat = slice(plane * AREA + k * STEP, plane * AREA + k * STEP + STEP)
            for at in range(0, HID2, 128):
                lanes = slice(at, at + 128)
                active, slope = gelu_pair(hid_ref[plane % 2, rows, lanes] + hid_bias[:, lanes])
                u_ref[flat, lanes] = active.astype(bf16)
                g_ref[flat, lanes] = slope.astype(bf16)
        out = product(u_ref[plane_rows(plane)], w2_ref[...]) + out_bias
        zed = jnp.where(inv_ref[plane] > 0.0, mix_ref[plane] + scale2 * out, 0.0)
        zed_ref[plane, LINE : LINE + AREA] = rounded(zed)

    def patches(k, carry):
        rows = step_rows(k)
        taps = []
        for ky in range(3):
            pr = (0 if ky == 1 else 1) * 2
            source = step_rows(k, 0 if ky == 0 else 1)
            even = zed_ref[pr, source]
            odd = zed_ref[pr + 1, source]
            taps.append((from_left(odd), even, odd))
        for ky in range(3):
            for kx in range(3):
                at = (3 * ky + kx) * C2
                tap = taps[ky][kx]
                if ky != kx:
                    tap = jnp.where(flipped, taps[kx][ky], tap)
                patch_ref[rows, at : at + C2] = tap.astype(bf16)
        return carry

    sweep(patches, 0)
    e_ref[...] = product(patch_ref[...], we_ref[...])

    def embed(k, carry):
        total, square = carry
        rows = step_rows(k)
        share = shape.share3(k)
        inv3_ref[rows] = share
        out = jnp.where(widen(share) > 0.0, e_ref[rows] + embed_bias, 0.0)
        e_ref[rows] = out
        return (total + fold(out), square + fold(out * out))

    total, square = sweep(embed, (nothing3, nothing3))
    mean3, scaling3 = norm_terms(total, square, count_three)
    factor3 = scaling3 * gain3
    shift3 = bias3 - mean3 * scaling3 * gain3

    def window_cols3(k, carry):
        rows = step_rows(k)
        normal = rounded(affine(e_ref[rows], factor3, shift3))
        masked = jnp.where(widen(inv3_ref[rows]) > 0.0, normal, 0.0)
        col3_ref[step_rows(k, 1)] = masked + from_left(masked) + from_right(masked)
        return carry

    sweep(window_cols3, 0)

    def row_windows3(k):
        return col3_ref[step_rows(k)] + col3_ref[step_rows(k, 1)] + col3_ref[step_rows(k, 2)]

    def mix3(k, carry):
        total, square = carry
        rows = step_rows(k)
        values = e_ref[rows]
        share = widen(inv3_ref[rows])
        pooled = row_windows3(k) * share - rounded(affine(values, factor3, shift3))
        pooled = jnp.where(share > 0.0, pooled, 0.0)
        mixed = values + scale3 * pooled
        pool3_ref[rows] = pooled
        mix3_ref[rows] = mixed
        return (total + fold(mixed), square + fold(mixed * mixed))

    total, square = sweep(mix3, (nothing3, nothing3))
    mean4, scaling4 = norm_terms(total, square, count_three)
    factor4 = scaling4 * gain4
    shift4 = bias4 - mean4 * scaling4 * gain4
    normal4 = (spread(scaling4, WIDE), spread(-mean4 * scaling4, WIDE))

    def prepare3(k, d_bias):
        rows = step_rows(k)
        h3_ref[rows] = affine(mix3_ref[rows], factor4, shift4).astype(bf16)
        goal = goal_ref[0, rows].astype(f32)
        goal = jnp.where(widen(inv3_ref[rows]) > 0.0, goal, 0.0)
        goal = scale4 * goal
        dy3_ref[rows] = goal.astype(bf16)
        return d_bias + fold(goal)

    acc_three[7] += sweep(prepare3, nothing3)

    def keep(which, value, row=0, col=0):
        if pairs == 1:
            pack_part(which, value, row, col)
        else:
            ref = grads[which]
            place = (slice(row, row + value.shape[0]), slice(col, col + value.shape[1]))

            @pl.when(pair == 0)
            def _():
                ref[place] = value

            @pl.when(pair > 0)
            def _():
                ref[place] += value

    def begin_chunk(at):
        lanes = slice(at, at + 256)
        hid3_ref[:, lanes] = product(h3_ref[...], w3_ref[:, lanes])
        dhid3_ref[:, lanes] = product_nt(dy3_ref[...], w4_ref[lanes])

    begin_chunk(0)
    for at in range(0, HID3, 256):
        if at + 256 < HID3:
            begin_chunk(at + 256)
        for lane in (at, at + 128):
            lanes = slice(lane, lane + 128)
            total = nothing
            for k in range(STEPS):
                rows = step_rows(k)
                active, slope = gelu_pair(hid3_ref[rows, lanes] + hid_bias3[:, lanes])
                u3_ref[rows, lanes] = active.astype(bf16)
                change = slope * dhid3_ref[rows, lanes]
                g3_ref[rows, lanes] = change.astype(bf16)
                total = total + fold(change)
            acc_hid_three[:, lanes] += total
        lanes = slice(at, at + 256)
        out = product(u3_ref[:, lanes], w4_ref[lanes])
        d_low = product_nt(g3_ref[:, lanes], w3_ref[:, lanes])
        result_ref[0] = out if at == 0 else result_ref[0] + out
        dx3_ref[...] = d_low if at == 0 else dx3_ref[...] + d_low
        keep(3, product_tn(h3_ref[...], g3_ref[:, lanes]), col=at)
        keep(4, product_tn(u3_ref[:, lanes], dy3_ref[...]), row=at)

    def finish3(k, carry):
        d_scale, d_shift, d_gain = carry
        rows = step_rows(k)
        valid = widen(inv3_ref[rows]) > 0.0
        mixed = mix3_ref[rows]
        out = jnp.where(valid, result_ref[0, rows] + out_bias3, 0.0)
        result_ref[0, rows] = mixed + scale4 * out
        d_scale = d_scale + fold(out * goal_ref[0, rows].astype(f32))
        d_low = dx3_ref[rows]
        normal = affine(mixed, *normal4)
        return (d_scale, d_shift + fold(d_low), d_gain + fold(d_low * normal))

    d_scale, d_shift, d_gain = sweep(finish3, (nothing3, nothing3, nothing3))
    acc_three[6] += d_scale
    acc_three[5] += d_shift
    acc_three[4] += d_gain
    mean_shift = by_image(d_shift * gain4) / count_three
    mean_gain = by_image(d_gain * gain4) / count_three
    back_gain4 = scaling4 * gain4
    back_mean4 = spread(-scaling4 * mean_shift, WIDE)
    back_normal4 = spread(scaling4 * mean_gain, WIDE)

    def unmix3(k, d_scale):
        rows = step_rows(k)
        share = widen(inv3_ref[rows])
        valid = share > 0.0
        normal = affine(mix3_ref[rows], *normal4)
        back = affine(dx3_ref[rows], back_gain4, back_mean4) - scaled(normal, back_normal4)
        d_mixed = jnp.where(valid, back + goal_ref[0, rows].astype(f32), 0.0)
        dx3_ref[rows] = d_mixed
        d_scale = d_scale + fold(pool3_ref[rows] * d_mixed)
        weighted = scale3 * d_mixed * share
        col3_ref[step_rows(k, 1)] = weighted + from_left(weighted) + from_right(weighted)
        return d_scale

    acc_three[3] += sweep(unmix3, nothing3)
    normal3 = (spread(scaling3, WIDE), spread(-mean3 * scaling3, WIDE))

    def unpool3(k, carry):
        d_shift, d_gain = carry
        rows = step_rows(k)
        valid = widen(inv3_ref[rows]) > 0.0
        d_normal = jnp.where(valid, row_windows3(k) - scale3 * dx3_ref[rows], 0.0)
        pool3_ref[rows] = d_normal
        normal = affine(e_ref[rows], *normal3)
        return (d_shift + fold(d_normal), d_gain + fold(d_normal * normal))

    d_shift, d_gain = sweep(unpool3, (nothing3, nothing3))
    acc_three[2] += d_shift
    acc_three[1] += d_gain
    mean_shift = by_image(d_shift * gain3) / count_three
    mean_gain = by_image(d_gain * gain3) / count_three
    back_gain3 = scaling3 * gain3
    back_mean3 = spread(-scaling3 * mean_shift, WIDE)
    back_normal3 = spread(scaling3 * mean_gain, WIDE)

    def unnorm3(k, d_bias):
        rows = step_rows(k)
        valid = widen(inv3_ref[rows]) > 0.0
        normal = affine(e_ref[rows], *normal3)
        back = affine(pool3_ref[rows], back_gain3, back_mean3) - scaled(normal, back_normal3)
        low = jnp.where(valid, dx3_ref[rows] + back, 0.0).astype(bf16)
        dpre_ref[rows] = low
        return d_bias + fold(low.astype(f32))

    acc_three[0] += sweep(unnorm3, nothing3)
    keep(2, product_tn(patch_ref[...], dpre_ref[...]))
    dpatch_ref[0:AREA] = product_nt(dpre_ref[...], we_ref[...])
    dpatch_ref[AREA : AREA + LINE] = jnp.zeros((LINE, 9 * C2), f32)

    def gather_back(k, carry):
        rows = step_rows(k)

        def tap(ky, kx, source):
            at = (3 * ky + kx) * C2
            value = dpatch_ref[source, at : at + C2]
            if ky != kx:
                at = (3 * kx + ky) * C2
                value = jnp.where(flipped, dpatch_ref[source, at : at + C2], value)
            return value

        sources = []
        for ky in range(3):
            source = step_rows(k, 1 if ky == 0 else 0)
            sources.append(
                (tap(ky, 1, source), tap(ky, 2, source) + from_right(tap(ky, 0, source)))
            )
        for pc in range(2):
            for pr, value in ((0, sources[1][pc]), (1, sources[2][pc] + sources[0][pc])):
                plane = pr * 2 + pc
                valid = inv_ref[plane, rows] > 0.0
                back_ref[plane, rows] = jnp.where(valid, rounded(value), 0.0)
        return carry

    sweep(gather_back, 0)

    normal2 = (spread(scaling2, C2), spread(-mean2 * scaling2, C2))

    def begin_back(plane):
        goal = scale2 * back_ref[plane]
        dy_ref[plane_rows(plane)] = goal.astype(bf16)
        hid_ref[plane % 2] = product_nt(goal.astype(bf16), w2_ref[...])
        return fold(goal)

    d_out_bias = begin_back(0)
    d_shift, d_gain = nothing, nothing
    sums = [nothing] * (HID2 // 128)
    new_gw1, new_gw2 = None, None
    for plane in range(4):
        if plane < 3:
            d_out_bias = d_out_bias + begin_back(plane + 1)
        for k in range(STEPS):
            rows = step_rows(k)
            part = slice(plane * AREA + k * STEP, plane * AREA + k * STEP + STEP)
            for n, at in enumerate(range(0, HID2, 128)):
                lanes = slice(at, at + 128)
                change = g_ref[part, lanes].astype(f32) * hid_ref[plane % 2, rows, lanes]
                g_ref[part, lanes] = change.astype(bf16)
                sums[n] = sums[n] + fold(change)
        flat = plane_rows(plane)
        d_low = product_nt(g_ref[flat], w1_ref[...])
        dx_ref[plane] = d_low
        d_shift = d_shift + fold(d_low)
        d_gain = d_gain + fold(d_low * affine(mix_ref[plane], *normal2))
        part_gw1 = product_tn(h_ref[flat], g_ref[flat])
        part_gw2 = product_tn(dy_ref[flat], u_ref[flat])
        new_gw1 = part_gw1 if plane == 0 else new_gw1 + part_gw1
        new_gw2 = part_gw2 if plane == 0 else new_gw2 + part_gw2
    new_gw2 = new_gw2.T
    for n, value in enumerate(sums):
        acc_hid_two[:, n * 128 : n * 128 + 128] += value
    acc_two[6] += d_out_bias
    acc_two[4] += d_shift
    acc_two[3] += d_gain
    mean_out[0, 0] = spread(by_image(d_shift * gain2) / count_two, 128)
    mean_out[0, 1] = spread(by_image(d_gain * gain2) / count_two, 128)
    keep(0, new_gw1)
    keep(1, new_gw2)
    d_scale = fold(w2_ref[...].astype(f32) * new_gw2) + out_bias * d_out_bias
    acc_two[5] += d_scale / scale2

    def finish():
        if pairs > 1:
            for which, ref in enumerate(grads):
                pack_part(which, ref[...])

        def filler(number, carry):
            put_block(number, jnp.zeros((HALF, 128), bf16))
            return carry

        lax.fori_loop(USED, slots, filler, 0)

        flat_ref[...] = jnp.zeros(flat_ref.shape, f32)

        def put(at, total, length):
            if at % 128:
                room = jnp.zeros((8, 128), f32)
                if total.shape[1] < length + BS:
                    total = jnp.concatenate([total, room], axis=1)
                total = pltpu.roll(total, BS, 1)
            whole = jnp.sum(total, axis=0, keepdims=True)
            done = -(at % 128)
            row = at // 128
            lane = 0
            while done < length:
                first = max(0, -done)
                last = min(128, length - done)
                flat_ref[row : row + 1, first:last] = whole[:, lane + first : lane + last]
                done += 128
                lane += 128
                row += 1

        at = 3 * C2
        for n in range(3, 6):
            put(at, acc_two[n], C2)
            at += C2
        put(at, acc_hid_two[...], HID2)
        at += HID2
        put(at, acc_two[6], C2)
        at += C2
        for n in range(7):
            put(at, acc_three[n], C3)
            at += C3
        put(at, acc_hid_three[...], HID3)
        at += HID3
        put(at, acc_three[7], C3)

    at_pair(pairs - 1, finish)


def run_main(places, place, buckets, state, goal, vec, weights, strip_count):
    pairs = goal.shape[0]
    slots = places[0].shape[0]
    half = slots // 2 + 1
    if pairs == 1:
        state = held_in(pltpu.VMEM, *state)
    weights = held_in(pltpu.VMEM, *weights)
    _, inv, _, mix, stat = state
    state_shapes = [STATE[1], STATE[3], STATE[4]]
    wide_f32 = pltpu.VMEM((AREA, WIDE), f32)
    wide_bf16 = pltpu.VMEM((AREA, WIDE), bf16)
    scratch = [
        pltpu.VMEM((4, AREA + LINE, C2), f32),
        pltpu.VMEM((2, AREA, HID2), f32),
        pltpu.VMEM((4 * AREA, HID2), bf16),
        pltpu.VMEM((4 * AREA, HID2), bf16),
        pltpu.VMEM((4 * AREA, C2), bf16),
        pltpu.VMEM((4 * AREA, C2), bf16),
        pltpu.VMEM((AREA, 9 * C2), bf16),
        pltpu.VMEM((AREA + LINE, 9 * C2), f32),
        pltpu.VMEM((AREA, 128), f32),
        wide_f32,
        pltpu.VMEM((AREA + 2 * LINE, WIDE), f32),
        wide_f32,
        wide_f32,
        wide_f32,
        pltpu.VMEM((AREA, HID3), f32),
        pltpu.VMEM((AREA, HID3), f32),
        pltpu.VMEM((AREA, HID3), bf16),
        pltpu.VMEM((AREA, HID3), bf16),
        wide_bf16,
        wide_bf16,
        wide_bf16,
        *[pltpu.VMEM(shape if pairs > 1 else (8, 128), f32) for shape in WEIGHTS],
        pltpu.VMEM((7, 8, C2), f32),
        pltpu.VMEM((8, HID2), f32),
        pltpu.VMEM((8, 8, WIDE), f32),
        pltpu.VMEM((8, HID3), f32),
    ]
    out_shapes = [(half, HALF, 128), (half, HALF, 128), (VEC_BLOCKS * HALF, 128)]
    make = pltpu.VMEM if pairs == 1 else jax.ShapeDtypeStruct
    return pl.pallas_call(
        functools.partial(main_kernel, pairs, strip_count, slots),
        grid=() if pairs == 1 else (pairs,),
        in_specs=[SMEM] * 4
        + pair_specs(pairs, state_shapes + [goal.shape[1:]], pl.Buffered(1))
        + whole_specs(pairs, [vec.shape])
        + [VMEM_BLOCK] * 5,
        out_specs=pair_specs(pairs, [(AREA, WIDE)] + BACK) + whole_specs(pairs, out_shapes),
        out_shape=pair_arrays(pairs, [(AREA, WIDE)] + BACK, [f32] * 4)
        + [make(shape, kind) for shape, kind in zip(out_shapes, (bf16, bf16, f32))],
        scratch_shapes=scratch,
        compiler_params=pltpu.CompilerParams(
            vmem_limit_bytes=(40 if pairs == 1 else 56) * 1024 * 1024,
        ),
        name="blocks",
    )(*places, place, buckets, inv, mix, stat, goal, vec, *weights)


def exit_kernel(
    pairs,
    strip_count,
    place_ref,
    bucket_ref,
    x_in,
    inv_in,
    pool_in,
    mix_in,
    stat_in,
    zed_in,
    dx_in,
    mean_in,
    flat_ref,
    vec_ref,
    payload_hbm,
    vector_ref,
    payload_ref,
    image_ref,
    col_ref,
    dx_ref,
    back_ref,
    acc_ref,
    sem,
):
    pair = pl.program_id(0) if pairs > 1 else 0
    x_ref, inv_ref, pool_ref, mix_ref, stat_ref, zed_ref, low_ref, mean_ref = (
        ref.at[0] for ref in (x_in, inv_in, pool_in, mix_in, stat_in, zed_in, dx_in, mean_in)
    )
    bucket_of = bucket_reader(place_ref, bucket_ref, strip_count)
    shape = Geometry(bucket_of, pair)
    count_two = shape.count_two
    gain1, bias1, scale1, gain2 = (vec_ref[n : n + 1] for n in range(4))
    mean1, scaling1, mean2, scaling2 = (stat_ref[n] for n in range(4))
    normal2 = (scaling2, -mean2 * scaling2)
    clear_edges(col_ref)
    nothing = jnp.zeros((8, C2), f32)
    back_gain2 = scaling2 * gain2
    back_mean2 = -scaling2 * mean_ref[0]
    back_normal2 = scaling2 * mean_ref[1]

    if pairs > 1:

        @pl.when(pair == 0)
        def _():
            acc_ref[...] = jnp.zeros(acc_ref.shape, f32)

    def add_up(n, total):
        acc_ref[n] = total if pairs == 1 else acc_ref[n] + total

    def unmix(k, d_scale):
        rows = step_rows(k)
        for pr in range(2):
            weighted = []
            for pc in range(2):
                plane = pr * 2 + pc
                share = inv_ref[plane, rows]
                normal = affine(mix_ref[plane, rows], *normal2)
                back = affine(low_ref[plane, rows], back_gain2, back_mean2)
                back = back - scaled(normal, back_normal2)
                d_mixed = jnp.where(share > 0.0, zed_ref[plane, rows] + back, 0.0)
                dx_ref[plane, rows] = d_mixed
                d_scale = d_scale + fold(pool_ref[plane, rows] * d_mixed)
                weighted.append(scale1 * d_mixed * share)
            put_col_windows(col_ref, pr, k, *weighted)
        return d_scale

    add_up(2, sweep(unmix, nothing))
    normal1 = (spread(scaling1, C2), spread(-mean1 * scaling1, C2))

    def unpool(k, carry):
        d_shift, d_gain = carry
        rows = step_rows(k)
        for pc in range(2):
            windows = row_windows(col_ref, pc, k)
            for pr in range(2):
                plane = pr * 2 + pc
                valid = inv_ref[plane, rows] > 0.0
                d_normal = windows[pr] - scale1 * dx_ref[plane, rows]
                d_normal = jnp.where(valid, d_normal, 0.0)
                back_ref[plane, rows] = d_normal
                normal = affine(x_ref[plane, rows], *normal1)
                d_shift = d_shift + fold(d_normal)
                d_gain = d_gain + fold(d_normal * normal)
        return (d_shift, d_gain)

    d_shift, d_gain = sweep(unpool, (nothing, nothing))
    add_up(1, d_shift)
    add_up(0, d_gain)
    mean_shift = by_image(d_shift * gain1) / count_two
    mean_gain = by_image(d_gain * gain1) / count_two
    back_gain1 = scaling1 * gain1
    back_mean1 = spread(-scaling1 * mean_shift, C2)
    back_normal1 = spread(scaling1 * mean_gain, C2)

    def unnorm(k, carry):
        rows = step_rows(k)
        for plane in range(4):
            normal = affine(x_ref[plane, rows], *normal1)
            back = affine(back_ref[plane, rows], back_gain1, back_mean1)
            back = back - scaled(normal, back_normal1)
            valid = inv_ref[plane, rows] > 0.0
            dx_ref[plane, rows] = jnp.where(valid, dx_ref[plane, rows] + back, 0.0)
        return carry

    sweep(unnorm, 0)

    def give_back(plane, here, spot, there):
        image_ref[spot, there] = dx_ref[plane, here]

    image_ref[...] = jnp.zeros(image_ref.shape, f32)
    each_image(bucket_of, pair, give_back)

    for spot in range(2 * STRIPS):
        target = strip_place(pair, spot, strip_count)
        for within in range(SR):
            rows = slice(within * CW, within * CW + CW)
            payload_ref[target, within] = image_ref[spot, rows].astype(bf16)

    def finish():
        copy = pltpu.make_async_copy(payload_ref, payload_hbm, sem)
        copy.start()
        vector_ref[...] = flat_ref[...]
        for n in range(3):
            vector_ref[n : n + 1] = jnp.sum(acc_ref[n], axis=0, keepdims=True)
        copy.wait()

    if pairs == 1:
        finish()
    else:
        pl.when(pair == pairs - 1)(finish)


def run_exit(place, buckets, state, back, flat, vec, strip_count):
    pairs = strip_count // 8
    payload = (strip_count, SR, CW, C2)
    make = pltpu.VMEM if pairs == 1 else jax.ShapeDtypeStruct
    plane_f32 = pltpu.VMEM((4, AREA, C2), f32)
    arrays = [*state, *back]
    if pairs == 1:
        arrays = held_in(pltpu.VMEM, *arrays)
    return pl.pallas_call(
        functools.partial(exit_kernel, pairs, strip_count),
        grid=() if pairs == 1 else (pairs,),
        in_specs=[SMEM] * 2
        + pair_specs(pairs, STATE + BACK, pl.Buffered(1))
        + whole_specs(pairs, [flat.shape, vec.shape]),
        out_specs=[HBM] + whole_specs(pairs, [flat.shape]),
        out_shape=[pltpu.HBM(payload, bf16), make(flat.shape, f32)],
        scratch_shapes=[
            pltpu.VMEM(payload, bf16),
            pltpu.VMEM((2 * STRIPS, STRIP_ROWS, C2), f32),
            pltpu.VMEM((4, AREA + 2 * LINE, C2), f32),
            plane_f32,
            plane_f32,
            pltpu.VMEM((3, 8, C2), f32),
            pltpu.SemaphoreType.DMA,
        ],
        compiler_params=roomy(8 if pairs == 1 else 40),
        name="exit",
    )(place, buckets, *arrays, flat, vec)


def dense_blocks(values):
    return jnp.concatenate([values[:, :HALF], values[:, HALF:]], axis=2).astype(bf16)


def pack_kernel(master_ref, dense_ref):
    dense_ref[...] = dense_blocks(master_ref[...])


def pack(master):
    owned = master.shape[0]
    return pl.pallas_call(
        pack_kernel,
        out_shape=jax.ShapeDtypeStruct((owned, HALF, 2 * BS), bf16),
        name="pack",
    )(master)


def pack_pieces_kernel(place_ref, master_hbm, pixel_hbm, *refs):
    out_refs, (wide_ref, master_ref, pixel_ref, sem) = refs[:-4], refs[-4:]
    owned = master_ref.shape[0]
    slots = pixel_ref.shape[2]
    copies = [pltpu.make_async_copy(pixel_hbm, pixel_ref, sem.at[0])]
    parts = [(0, owned // 2), (owned // 2, owned - owned // 2)]
    for n, part in enumerate(parts):
        copies.append(
            pltpu.make_async_copy(
                master_hbm.at[pl.ds(*part)], master_ref.at[pl.ds(*part)], sem.at[1 + n]
            )
        )
    for copy in copies:
        copy.start()
    copies[0].wait()

    def widen_row(row, carry):
        start = pl.multiple_of(row * CW * slots, 8)
        values = pixel_ref[row].astype(f32).reshape(CW * slots, C2)
        wide_ref[pl.ds(start, CW * slots)] = values
        return carry

    lax.fori_loop(0, SR, widen_row, 0)
    for k, ref in enumerate(out_refs):
        for other in range(2):
            slot = place_ref[0] ^ (2 * k + other)
            first = other * (ref.shape[0] - STRIP_ROWS)
            strip = wide_ref[pl.ds(slot, STRIP_ROWS, stride=slots)]
            ref[first : first + STRIP_ROWS] = strip.astype(bf16)
    for (first, count), copy in zip(parts, copies[1:]):
        copy.wait()
        dense = dense_blocks(master_ref[first : first + count]).reshape(count * HALF, 2 * BS)
        start = STRIP_ROWS + first * HALF
        for ref in out_refs[:3]:
            ref[start : start + count * HALF] = dense


def pack_pieces(place, master, pixels):
    slots = pixels.shape[2]
    rows = master.shape[0] * HALF
    shapes = [(rows + 2 * STRIP_ROWS, 2 * BS)] * 3 + [(2 * STRIP_ROWS, 2 * BS)]
    return pl.pallas_call(
        pack_pieces_kernel,
        in_specs=[SMEM] + [HBM] * 2,
        out_specs=[VMEM_BLOCK] * 4,
        out_shape=[pltpu.VMEM(shape, bf16) for shape in shapes],
        scratch_shapes=[
            pltpu.VMEM((STRIP_ROWS * slots, C2), f32),
            pltpu.VMEM(master.shape, f32),
            pltpu.VMEM(pixels.shape, bf16),
            pltpu.SemaphoreType.DMA((3,)),
        ],
        compiler_params=roomy(12),
        name="pack",
    )(place, *held_in(pltpu.HBM, master, pixels))


def fold_pair_kernel(near_ref, got_ref, own_ref, *part_refs):
    share = own_ref.shape[0]

    def one(n, carry):
        own_ref[n] = near_ref[n].astype(f32) + got_ref[n].astype(f32)
        for k, ref in enumerate(part_refs):
            here = (k + 1) * share + n
            ref[n] = near_ref[here] + got_ref[here]
        return carry

    lax.fori_loop(0, share, one, 0, unroll=4)


def fold_pair(near, got, groups):
    shape = ((near.shape[0] - 1) // groups,) + near.shape[1:]
    return pl.pallas_call(
        fold_pair_kernel,
        in_specs=[VMEM_BLOCK] * 2,
        out_specs=[VMEM_BLOCK] * groups,
        out_shape=[pltpu.VMEM(shape, f32)] + [pltpu.VMEM(shape, bf16)] * (groups - 1),
        compiler_params=roomy(4),
        name="fold_pair",
    )(*held_in(pltpu.VMEM, near, got))


def fold_tile_kernel(pieces, spot_ref, *refs):
    piece_refs, refs = refs[:pieces], refs[pieces:]
    vector_refs, refs = refs[:pieces], refs[pieces:]
    out_refs, sum_ref = refs[:-1], refs[-1]
    groups = len(out_refs)
    share = out_refs[0].shape[0]
    owned = piece_refs[0].shape[0]
    total = vector_refs[0][...]
    for ref in vector_refs[1:]:
        total = total + ref[...]
    for n in range(sum_ref.shape[0]):
        sum_ref[n] = jnp.zeros((HALF, 128), f32)
    for n in range(VEC_BLOCKS):
        sum_ref[n] = total[n * HALF : (n + 1) * HALF]

    def one(n, carry):
        for k, out_ref in enumerate(out_refs):
            number = lax.rem(spot_ref[0] + k, groups) * share + n
            block = jnp.minimum(number, owned - 1)
            total = piece_refs[0][block].astype(f32)
            for ref in piece_refs[1:]:
                total = total + ref[block].astype(f32)
            rest = sum_ref[jnp.maximum(number - owned, 0)]
            out_ref[n] = jnp.where(number < owned, total, rest).astype(out_ref.dtype)
        return carry

    lax.fori_loop(0, share, one, 0, unroll=share <= 16)


def fold_tile(spot, pieces, vectors, extra, groups):
    shape = ((pieces[0].shape[0] + extra) // groups,) + pieces[0].shape[1:]
    return pl.pallas_call(
        functools.partial(fold_tile_kernel, len(pieces)),
        in_specs=[SMEM] + [VMEM_BLOCK] * (len(pieces) + len(vectors)),
        out_specs=[VMEM_BLOCK] * groups,
        out_shape=[pltpu.VMEM(shape, f32)] + [pltpu.VMEM(shape, bf16)] * (groups - 1),
        scratch_shapes=[pltpu.VMEM((extra, HALF, 128), f32)],
        compiler_params=roomy(8),
        name="fold_tile",
    )(spot, *held_in(pltpu.VMEM, *pieces, *vectors))


def fold_batch_kernel(owned, vector_weight, spot_ref, *refs):
    part_refs, (total_ref, norm_ref) = refs[:-2], refs[-2:]
    share = total_ref.shape[0]
    square = jnp.zeros((8, 128), f32)
    for n in range(share):
        total = part_refs[0][n].astype(f32)
        for ref in part_refs[1:]:
            total = total + ref[n].astype(f32)
        total_ref[n] = total.astype(bf16)
        weight = jnp.where(spot_ref[0] * share + n < owned, 1.0, vector_weight)
        square = square + weight * fold(total * total)
    square = jnp.sum(jnp.sum(square, axis=1, keepdims=True), axis=0, keepdims=True)
    norm_ref[...] = jnp.broadcast_to(square[None], norm_ref.shape)


def fold_batch(spot, parts, owned, tile_count):
    count = tile_count * len(parts)
    return pl.pallas_call(
        functools.partial(fold_batch_kernel, owned, 1.0 / tile_count),
        in_specs=[SMEM] + [VMEM_BLOCK] * len(parts),
        out_specs=[VMEM_BLOCK] * 2,
        out_shape=[pltpu.VMEM(parts[0].shape, bf16), pltpu.VMEM((count, 1, 128), f32)],
        name="fold_batch",
    )(spot, *held_in(pltpu.VMEM, *parts))


def update_kernel(owned, groups, spot_ref, norm_ref, *refs):
    quarters, refs = refs[:groups], refs[groups:]
    stat_hbm, out_hbm, (vector_ref, clip_ref), refs = refs[:5], refs[5:10], refs[10:12], refs[12:]
    stat_refs, out_refs, (in_sem, out_sem) = refs[:5], refs[5:10], refs[10:]
    master_ref, left_stat_ref, right_stat_ref, left_root_ref, right_root_ref = stat_refs
    grad_ref, left_ref, right_ref, new_ref, copy_ref = out_refs
    share = quarters[0].shape[0]
    spans = spans_of(owned)

    def copies_of(sources, targets, sems):
        return [
            [
                pltpu.make_async_copy(
                    source.at[pl.ds(*span)], target.at[pl.ds(*span)], sems.at[5 * n + k]
                )
                for k, (source, target) in enumerate(zip(sources, targets))
            ]
            for n, span in enumerate(spans)
        ]

    copies_in = copies_of(stat_hbm, stat_refs, in_sem)
    copies_out = copies_of(out_refs, out_hbm, out_sem)
    for copies in copies_in:
        for copy in copies:
            copy.start()
    norm = jnp.sqrt(jnp.sum(norm_ref[...], axis=0))
    factor = jnp.minimum(1.0, clip_limit / norm)
    left_half = lax.broadcasted_iota(jnp.int32, (HALF, 128), 1) < BS

    def summed(number):
        source = number // share
        local = number - source * share
        turn = lax.rem(spot_ref[0] - source + groups, groups)
        value = quarters[0][local].astype(f32)
        for k in range(1, groups):
            value = jnp.where(turn == k, quarters[k][local].astype(f32), value)
        return value * factor

    def side_by_side(first, count):
        sides = []
        for n in range(first, first + count, 2):
            dense = summed(n)
            turned = pltpu.roll(dense, BS, 1)
            if n + 1 < first + count:
                second = summed(n + 1)
                top = jnp.where(left_half, dense, pltpu.roll(second, BS, 1))
                low = jnp.where(left_half, turned, second)
                side = jnp.concatenate([top, low], axis=0)
                grad_ref[n + 1] = pltpu.roll(side, BS, 1)[:, :BS]
            else:
                side = jnp.concatenate([dense, turned], axis=0)[:, :BS]
            grad_ref[n] = side[:, :BS]
            sides.append(side.astype(bf16))
        return jnp.concatenate(sides, axis=1)

    def diagonal_of(count):
        order = (count * BS, count * BS)
        return lax.broadcasted_iota(jnp.int32, order, 0) // BS == (
            lax.broadcasted_iota(jnp.int32, order, 1) // BS
        )

    clip_ref[...] = norm
    for n in range(vector_ref.shape[0]):
        vector_ref[n] = summed(owned + n)
    for (first, length), arriving, leaving in zip(spans, copies_in, copies_out):
        parts = [(n, min(4, first + length - n)) for n in range(first, first + length, 4)]
        wides = [side_by_side(*part) for part in parts]
        tall = [
            jnp.where(diagonal_of(count), jnp.concatenate([wide] * count, axis=0), 0.0)
            for (_, count), wide in zip(parts, wides)
        ]
        lefts = [product_nt(one, wide) for one, wide in zip(tall, wides)]
        rights = [product_tn(wide, wide) for wide in wides]
        for copy in arriving:
            copy.wait()
        stepped = []
        for (start, count), wide in zip(parts, wides):
            roots = left_root_ref[pl.ds(start, count)].reshape(count * BS, BS).astype(bf16)
            stepped.append(product(roots, wide))
        for (start, count), left, right in zip(parts, lefts, rights):
            here = pl.ds(start, count)
            left_ref[here] = 0.5 * left_stat_ref[here] + 0.5 * left.reshape(count, BS, BS)
            for n in range(count):
                at = n // 2 * 128
                block = right[n * BS : n * BS + BS, at : min(at + 128, count * BS)]
                if n % 2:
                    block = pltpu.roll(block, BS, 1)
                right_ref[start + n] = 0.5 * right_stat_ref[start + n] + 0.5 * block[:, :BS]
        for (start, count), value in zip(parts, stepped):
            here = pl.ds(start, count)
            value = jnp.where(diagonal_of(count), value, 0.0).astype(bf16)
            roots = right_root_ref[here].reshape(count * BS, BS).astype(bf16)
            value = product(value, roots).reshape(count, BS, BS)
            new = master_ref[here] - rate_matrix * value
            new_ref[here] = new
            copy_ref[here] = new.astype(bf16)
        for copy in leaving:
            copy.start()
    for leaving in copies_out:
        for copy in leaving:
            copy.wait()


def spans_of(owned):
    spans = []
    first = 0
    while first < owned:
        length = min(8 if first == 0 else 12, owned - first)
        spans.append((first, length))
        first += length
    return spans


def update(spot, norm, quarters, extra, *stats):
    shape = stats[0].shape
    groups = len(quarters)
    types = [f32] * 4 + [bf16]
    steps = len(spans_of(shape[0]))
    return pl.pallas_call(
        functools.partial(update_kernel, shape[0], groups),
        in_specs=[SMEM] + [VMEM_BLOCK] * (groups + 1) + [HBM] * 5,
        out_specs=[HBM] * 5 + [VMEM_BLOCK] * 2,
        out_shape=[pltpu.HBM(shape, kind) for kind in types]
        + [
            pltpu.VMEM((extra, HALF, 128), f32),
            pltpu.VMEM((1, 128), f32),
        ],
        scratch_shapes=[pltpu.VMEM(shape, f32)] * 5
        + [pltpu.VMEM(shape, kind) for kind in types]
        + [
            pltpu.SemaphoreType.DMA((5 * steps,)),
            pltpu.SemaphoreType.DMA((5 * steps,)),
        ],
        compiler_params=roomy(20),
        name="update",
    )(spot, *held_in(pltpu.VMEM, norm, *quarters), *held_in(pltpu.HBM, *stats))


def share_out(pieces, axis):
    return lax.all_to_all(pieces, axis, split_axis=0, concat_axis=0, tiled=True)


def swap(piece, distance):
    count = lax.axis_size("tile")
    return lax.ppermute(piece, "tile", [(i, i ^ distance) for i in range(count)])


def on_device(
    pixels,
    buckets,
    slot_owner_table,
    out_grad,
    master,
    left_stat,
    right_stat,
    left_root,
    right_root,
    vectors,
    moment,
):
    tile_count = lax.axis_size("tile")
    tile_place = lax.axis_index("tile")
    slot_count = pixels.shape[2]
    group_count = tile_count // STRIPS
    pairs = group_count // 2
    owned = master.shape[0]
    slots = owned * tile_count
    batch_count = lax.axis_size("batch")
    spot = lax.axis_index("batch").astype(jnp.int32).reshape(1)
    extra = extra_of(owned, batch_count)
    place = tile_place.astype(jnp.int32).reshape(1)
    paired = tile_count == 8
    numbers = jnp.arange(slots, dtype=jnp.int32)
    slot_of = jnp.sum(
        jnp.where(slot_owner_table[None, :] == numbers[:, None], numbers[None, :], 0), axis=1
    )
    if paired:
        owner = slot_of // owned
        apart = owner ^ tile_place
        apart = (apart & 1) * (tile_count // 2) + (apart >> 1)
        slot_of = slot_of + owned * (apart - owner)
    half = slots // 2
    near_place = jnp.where(slot_of < half, slot_of, half)
    far_place = jnp.where(slot_of < half, half, slot_of - half)
    vec = vectors.reshape(-1, 128)
    turned = lax.dynamic_index_in_dim(
        buckets.reshape(group_count, slot_count), tile_place, 1, keepdims=False
    ) >= 2
    flips = turned.reshape(-1, 1, 1, 1)
    goal = out_grad.reshape(2 * pairs, H3, W3, C3)
    goal = jnp.where(flips, goal.transpose(0, 2, 1, 3), goal)[:, :LINES]
    goal = goal.reshape(pairs, 2, LINES, W3, C3).transpose(0, 2, 3, 1, 4)
    goal = goal.reshape(pairs, LINES, 2 * W3, C3)
    goal = jnp.pad(goal, ((0, 0), (0, 0), (0, LINE - 2 * W3), (0, WIDE - C3)))
    goal = goal.reshape(pairs, AREA, WIDE)

    if paired:
        own, for_x, for_y, for_both = pack_pieces(
            place, master, pixels[0, 0].transpose(1, 2, 0, 3)
        )
        goal, for_both = lax.optimization_barrier((goal, for_both))
        from_x, from_y, strips_both = swap(for_x, 2), swap(for_y, 4), swap(for_both, 6)
        near_half = (owned + 1) // 2
        middle = STRIP_ROWS + near_half * HALF
        first_half = swap(from_x[STRIP_ROWS:middle], 4)
        second_half = swap(from_y[middle : STRIP_ROWS + owned * HALF], 2)
        mine = [own, from_x, from_y, strips_both, first_half, second_half]
        both = mine + [swap(piece, 1) for piece in mine]
        strips = both[:4] + both[6:10]
        pieces = [both[n] for n in (0, 1, 2, 4, 5, 6, 7, 8, 10, 11)]
        spans = [(STRIP_ROWS, owned)] * 3 + [(0, near_half), (0, owned - near_half)]
        spans = spans * 2
    else:
        pieces = [lax.all_gather(pack(master), "tile", axis=0, tiled=True).reshape(-1, 2 * BS)]
        spans = [(0, slots)]
        strips = share_out(pixels.reshape(tile_count, STRIP, C2), "tile")
        strips = [jnp.pad(strips, ((0, 0), (0, STRIP_ROWS - STRIP), (0, 0)))]

    weights = run_unpack(slot_of, pieces, spans)
    state = run_entry(place, buckets, strips, vec, tile_count)
    result, *back, near, far, flat = run_main(
        (near_place, far_place),
        place,
        buckets,
        state,
        goal,
        vec,
        weights,
        tile_count,
    )
    pixel_back, vector = run_exit(place, buckets, state, back, flat, vec, tile_count)
    if paired:
        own, *parts = fold_pair(near, swap(far, 1), tile_count // 2)
        pieces = [own] + [swap(part, 2 * k + 2) for k, part in enumerate(parts)]
        vector, _ = lax.optimization_barrier((vector, parts[0]))
        vector = vector + swap(vector, 1)
        vectors_in = [vector] + [swap(vector, 2 * k) for k in range(1, tile_count // 2)]
    else:
        outgoing = jnp.concatenate([near[:half], far[:half]], axis=0)
        pieces = list(share_out(outgoing.reshape(tile_count, owned, HALF, 128), "tile"))
        vectors_in = list(lax.all_gather(vector, "tile"))
    result, pieces[1] = lax.optimization_barrier((result, pieces[1]))
    result = result.reshape(pairs, LINES, LINE, WIDE)[:, :, : 2 * W3, :C3]
    result = result.reshape(pairs, LINES, W3, 2, C3).transpose(0, 3, 1, 2, 4)
    result = result.reshape(2 * pairs, LINES, W3, C3)
    result = jnp.pad(result, ((0, 0), (0, H3 - LINES), (0, 0), (0, 0)))
    result = jnp.where(flips, result.transpose(0, 2, 1, 3), result)
    result = result.reshape(out_grad.shape)
    result = with_layout_constraint(result, Layout(major_to_minor=(0, 1, 2, 4, 5, 3, 6)))
    result, vectors_in[0] = lax.optimization_barrier((result, vectors_in[0]))
    own, *parts = fold_tile(spot, pieces, vectors_in, extra, batch_count)
    pixel_back, parts[0] = lax.optimization_barrier((pixel_back, parts[0]))
    returned = share_out(pixel_back, "tile")
    parts = [
        lax.ppermute(part, "batch", [(i, (i + k + 1) % batch_count) for i in range(batch_count)])
        for k, part in enumerate(parts)
    ]
    quarter, norm = fold_batch(spot, [own] + parts, owned, tile_count)
    returned, norm = lax.optimization_barrier((returned, norm))
    norm = share_out(norm, ("batch", "tile"))
    returned = returned.astype(f32).reshape(pixels.shape)
    returned = with_layout_constraint(returned, Layout(major_to_minor=(0, 1, 3, 4, 2, 5)))
    returned, norm = lax.optimization_barrier((returned, norm))
    quarters = [quarter] + [
        lax.ppermute(quarter, "batch", [(i, (i + k) % batch_count) for i in range(batch_count)])
        for k in range(1, batch_count)
    ]
    block_grad, left_new, right_new, master_new, weight_copy, whole_vector, clip = update(
        spot, norm, quarters, extra, master, left_stat, right_stat, left_root, right_root
    )
    clip_norm = clip[0, 0]
    share = vectors.shape[0] // tile_count
    whole_vector = whole_vector.reshape(-1)
    vec_grad = lax.dynamic_slice_in_dim(whole_vector, tile_place * share, share, 0)
    vec_moment = moment + vec_grad * vec_grad
    own_vectors = lax.dynamic_slice_in_dim(vectors, tile_place * share, share, 0)
    vec_new = own_vectors - rate_vector * vec_grad / (jnp.sqrt(vec_moment) + eps_adagrad)
    return (
        result,
        returned,
        clip_norm,
        block_grad,
        left_new,
        right_new,
        master_new,
        weight_copy,
        vec_grad,
        vec_moment,
        vec_new,
    )


def solution(mesh):
    placed = (
        P("batch", "tile", None, None, None, None),
        P("batch"),
        P(),
        P("batch", "tile", None, None, None, None, None),
        P("tile", None, None),
        P("tile", None, None),
        P("tile", None, None),
        P("tile", None, None),
        P("tile", None, None),
        P(),
        P("tile"),
    )
    return jax.shard_map(
        on_device,
        mesh=mesh,
        in_specs=placed,
        out_specs=(
            P("batch", "tile", None, None, None, None, None),
            P("batch", "tile", None, None, None, None),
            P(),
            P("tile", None, None),
            P("tile", None, None),
            P("tile", None, None),
            P("tile", None, None),
            P("tile", None, None),
            P("tile"),
            P("tile"),
            P("tile"),
        ),
        check_vma=False,
    )
```
